32 devices in a mesh: rep: 8 (over z, x), exp: 4 (over y, core).
Axes of the slice: x: 2, y: 2, z: 4, core: 2. Of those that a mesh axis runs over, the one named last changes fastest.
Arguments:
- tokens: bfloat16 [8192, 1024], P(('rep', 'exp')), may hold values from -6 to 6
- cotangent: bfloat16 [8192, 1024], P(('rep', 'exp')), may hold values from -6 to 6
- seq_lengths: int32 [32], replicated, may hold values from 128 to 256, as said below
- deal: int32 [32], replicated, may hold values from 0 to 31, as said below
- routes: int32 [8192, 2], replicated, may hold values from 0 to 3, all different within a row; in each aligned block of 256 rows (0 to 255, 256 to 511, ...) at most 160 rows name the same one
- attn_qkv: float32 [1024, 3072], P('exp', 'rep'), may hold values from -0.1875 to 0.1875
- qkv_first: float32 [1024, 3072], P('exp', 'rep'), may hold values from -16 to 16
- qkv_second: float32 [1024, 3072], P('exp', 'rep'), may hold values from 0.73728 to 2.94912
- attn_out: float32 [1024, 1024], P('exp', 'rep'), may hold values from -0.75 to 0.75
- out_first: float32 [1024, 1024], P('exp', 'rep'), may hold values from -16 to 16
- out_second: float32 [1024, 1024], P('exp', 'rep'), may hold values from 0.73728 to 2.94912
- rel_bias: float32 [32, 16], replicated, may hold values from -3 to 3
- bias_first: float32 [32, 16], replicated, may hold values from -6 to 6
- bias_second: float32 [32, 16], replicated, may hold values from 0.08192 to 0.32768
- router: float32 [1024, 4], replicated, may hold values from -0.125 to 0.125
- router_first: float32 [1024, 4], replicated, may hold values from -512 to 512
- router_second: float32 [1024, 4], replicated, may hold values from 524.288 to 2097.152
- norm_gains: float32 [1024, 2], replicated, may hold values from 0.5 to 1.5
- gains_first: float32 [1024, 2], replicated, may hold values from -96 to 96
- gains_second: float32 [1024, 2], replicated, may hold values from 18.432 to 73.728
- expert_in: float32 [4, 1024, 5632], P('exp', 'rep'), may hold values from -0.1875 to 0.1875
- in_first: float32 [4, 1024, 5632], P('exp', 'rep'), may hold values from -12 to 12
- in_second: float32 [4, 1024, 5632], P('exp', 'rep'), may hold values from 0.36864 to 1.47456
- expert_out: float32 [4, 2816, 1024], P('exp', 'rep'), may hold values from -0.109375 to 0.109375
- down_first: float32 [4, 2816, 1024], P('exp', 'rep'), may hold values from -10 to 10
- down_second: float32 [4, 2816, 1024], P('exp', 'rep'), may hold values from 0.256 to 1.024
Outputs:
- block_out: bfloat16 [8192, 1024], P(('rep', 'exp'))
- grad_tokens: float32 [8192, 1024], P(('rep', 'exp'))
- new_qkv_first: float32 [1024, 3072], P('exp', 'rep')
- new_qkv_second: float32 [1024, 3072], P('exp', 'rep')
- new_attn_qkv: float32 [1024, 3072], P('exp', 'rep')
- new_out_first: float32 [1024, 1024], P('exp', 'rep')
- new_out_second: float32 [1024, 1024], P('exp', 'rep')
- new_attn_out: float32 [1024, 1024], P('exp', 'rep')
- new_bias_first: float32 [32, 16], replicated
- new_bias_second: float32 [32, 16], replicated
- new_rel_bias: float32 [32, 16], replicated
- new_router_first: float32 [1024, 4], replicated
- new_router_second: float32 [1024, 4], replicated
- new_router: float32 [1024, 4], replicated
- new_gains_first: float32 [1024, 2], replicated
- new_gains_second: float32 [1024, 2], replicated
- new_norm_gains: float32 [1024, 2], replicated
- new_in_first: float32 [4, 1024, 5632], P('exp', 'rep')
- new_in_second: float32 [4, 1024, 5632], P('exp', 'rep')
- new_expert_in: float32 [4, 1024, 5632], P('exp', 'rep')
- new_down_first: float32 [4, 2816, 1024], P('exp', 'rep')
- new_down_second: float32 [4, 2816, 1024], P('exp', 'rep')
- new_expert_out: float32 [4, 2816, 1024], P('exp', 'rep')
The draws below stay inside these ranges and needn't reach their ends.
Inputs may be any that keep to these rules, and one draw needn't show every extreme that they name: `seq_lengths`: one sequence has exactly 256 tokens. `deal`: a permutation that maps each aligned group of 4 consecutive sequences onto itself. The two experts of a slot differ; among the 512 routes of one sequence no expert is named more than 160 times, and in some sequence some expert exactly 160 times.
All inputs are finite; a program needn't handle non-finite values.
Results may differ from the reference program's by a relative error of at most 0.017.
Values may be sent and summed in bfloat16 or wider, within the bound.
A program may use at most 256 MiB of HBM per device.

```python
import math
import jax
import jax.numpy as jnp
import numpy as np
from jax import lax

D = 1024
HEADS = 16
HEAD_DIM = 64
FF = 2816
TOK_DEV = 256
BUCKETS = 32
STEP = 10
NSEQ = 32
TOKENS = 8192
EXPERTS = 4
CAP = 160
N_EXP = 4


def draw_seq_lengths(key, part):
    key = jax.random.fold_in(key, 11)
    value_key, pick_key = jax.random.split(key)
    drawn = jax.random.randint(value_key, (NSEQ,), TOK_DEV // 2, TOK_DEV + 1)
    picked = jax.random.randint(pick_key, (), 0, NSEQ)
    return jnp.where(jnp.arange(NSEQ) == picked, TOK_DEV, drawn).astype(jnp.int32)


def draw_deal(key, part):
    key = jax.random.fold_in(key, 23)
    group_count = NSEQ // N_EXP
    group_keys = jax.random.split(key, group_count)
    orders = jax.vmap(lambda one_key: jax.random.permutation(one_key, N_EXP))(group_keys)
    starts = jnp.arange(group_count, dtype=jnp.int32)[:, None] * N_EXP
    return (orders.astype(jnp.int32) + starts).reshape(-1).astype(jnp.int32)


def block_levels(rng, dims, pieces, least, largest):
    gain = 1.0
    for dim, parts in pieces:
        draws = jax.random.uniform(jax.random.fold_in(jax.random.fold_in(rng, 6), dim), (parts,), jnp.float32, least / len(pieces), largest / len(pieces))
        gain = gain * jnp.repeat(jnp.exp(draws), dims[dim] // parts).reshape((-1,) + (1,) * (len(dims) - 1 - dim))
    return gain


def routed_block(rng, own, number, rows, count, top, bound, skew):
    sequence = jax.random.permutation(rng, count)
    packed, ordinary = portions_of(count, rows * top, bound, skew, True), portions_of(count, rows * top, bound, skew, False)
    places = jnp.arange(count)

    def named(sizes, turn):
        used = int((sizes > 0).sum())
        fixed = max(1, used // 4)
        moved = fixed + (places - fixed + turn * (used - fixed)) % max(1, count - fixed)
        return jnp.zeros((count,), jnp.int32).at[sequence[jnp.where(places < fixed, places, moved)]].set(jnp.asarray(sizes, jnp.int32))

    sizes = jnp.where(number % 4 == 0, named(packed, number // 4), named(ordinary, number - number // 4 - 1))
    mixed = jax.random.permutation(jax.random.fold_in(own, 3), count)
    giver, sink = mixed[0:count // 2 * 2:2], mixed[1:count // 2 * 2:2]
    slack = jnp.minimum(sizes[giver] - 1, bound - sizes[sink]) // 2
    slack = jnp.where((giver == sequence[0]) | (sink == sequence[0]) | (sizes[sink] == 0), 0, jnp.maximum(slack, 0))
    moved = jax.random.randint(jax.random.fold_in(own, 4), (count // 2,), 0, 1 << 20) % (slack + 1)
    sizes = sizes.at[giver].add(-moved).at[sink].add(moved)
    items = jnp.searchsorted(jnp.cumsum(sizes), jnp.arange(rows * top), side="right").astype(jnp.int32)
    table = items.reshape(top, rows).T
    table = table[jax.random.permutation(jax.random.fold_in(own, 1), rows)]
    turn = jax.random.randint(jax.random.fold_in(own, 2), (rows, 1), 0, top)
    return jnp.take_along_axis(table, (jnp.arange(top)[None, :] + turn) % top, axis=1)


def portions_of(count, total, reach, slope, full):
    loads = [(1 << 20) // math.isqrt(standing ** slope) + 1 for standing in range(1, count + 1)]
    largest = reach if full else min(reach, max(-(-total // count), total * loads[0] // sum(loads)))
    least = 1 if total - largest >= count - 1 else 0
    holding, surplus = [largest] + [least] * (count - 1), total - largest - least * (count - 1)
    while surplus > 0:
        movable = [i for i in range(1, count) if holding[i] < largest] or [i for i in range(1, count) if holding[i] < reach]
        whole, budget = sum([loads[i] for i in movable]), surplus
        for i in movable:
            more = min(reach - holding[i], max(1, budget * loads[i] // whole), surplus)
            holding[i] = holding[i] + more
            surplus = surplus - more
    return np.array(holding)


def normal_values(own_key, dims, scale, most, cuts=(), kind=jnp.bfloat16):
    array = scale * jax.random.normal(own_key, dims, jnp.float32)
    if cuts:
        array = array * block_levels(own_key, dims, cuts, -0.22, 0.18)
    return jnp.clip(array, -most, most).astype(kind)


def setup_inputs(seed: int = 0) -> dict:
    key_list = jax.random.split(jax.random.key(seed), 27)
    tokens = normal_values(key_list[0], (TOKENS, D), 1.0, 6.0, ((0, 32),))
    cotangent = normal_values(key_list[1], (TOKENS, D), 1.0, 6.0, ((0, 32),))
    seq_lengths = draw_seq_lengths(jax.random.fold_in(key_list[26], 71), 0)
    deal = draw_deal(jax.random.fold_in(key_list[26], 71), 0)
    routes_keys = jax.random.split(jax.random.fold_in(key_list[4], 1), TOKENS // TOK_DEV)
    routes_turns = jax.random.permutation(jax.random.fold_in(key_list[4], 3), TOKENS // TOK_DEV)
    routes = jax.vmap(lambda own, number: routed_block(jax.random.fold_in(key_list[4], 2), own, number, TOK_DEV, EXPERTS, 2, CAP, 2))(routes_keys, routes_turns).reshape((TOKENS, 2))
    attn_qkv = normal_values(key_list[5], (D, 3 * D), D ** -0.5, 0.1875, ((0, 4), (1, 8)), jnp.float32)
    qkv_first = normal_values(key_list[6], (D, 3 * D), (0.033 * TOKENS ** 0.5), 16.0, ((0, 4), (1, 8)), jnp.float32)
    qkv_second = jnp.clip(jnp.exp(math.log(2.94912) - 1.3862944 * jax.random.uniform(key_list[7], (D, 3 * D), jnp.float32) ** block_levels(key_list[7], (D, 3 * D), ((0, 4), (1, 8)), -0.2, 0.2)), 0.73728, 2.94912)
    attn_out = normal_values(key_list[8], (D, D), (D // 16) ** -0.5, 0.75, ((0, 4), (1, 8)), jnp.float32)
    out_first = normal_values(key_list[9], (D, D), (0.033 * TOKENS ** 0.5), 16.0, ((0, 4), (1, 8)), jnp.float32)
    out_second = jnp.clip(jnp.exp(math.log(2.94912) - 1.3862944 * jax.random.uniform(key_list[10], (D, D), jnp.float32) ** block_levels(key_list[10], (D, D), ((0, 4), (1, 8)), -0.2, 0.2)), 0.73728, 2.94912)
    rel_bias = normal_values(key_list[11], (BUCKETS, HEADS), 0.5, 3.0, (), jnp.float32)
    bias_first = normal_values(key_list[12], (BUCKETS, HEADS), (0.011 * TOKENS ** 0.5), 6.0, (), jnp.float32)
    bias_second = jnp.clip(jnp.exp(jax.random.uniform(key_list[13], (BUCKETS, HEADS), jnp.float32, math.log(0.08192), math.log(0.32768))), 0.08192, 0.32768)
    router = normal_values(key_list[14], (D, EXPERTS), (2 * D) ** -0.5, 0.125, (), jnp.float32)
    router_first = normal_values(key_list[15], (D, EXPERTS), (0.0275 * (D * TOKENS) ** 0.5), 512.0, (), jnp.float32)
    router_second = jnp.clip(jnp.exp(jax.random.uniform(key_list[16], (D, EXPERTS), jnp.float32, math.log(524.288), math.log(2097.152))), 524.288, 2097.152)
    norm_gains = jnp.clip(1.0 + 0.1 * jax.random.normal(key_list[17], (D, 2), jnp.float32), 0.5, 1.5)
    gains_first = normal_values(key_list[18], (D, 2), (0.165 * TOKENS ** 0.5), 96.0, (), jnp.float32)
    gains_second = jnp.clip(jnp.exp(jax.random.uniform(key_list[19], (D, 2), jnp.float32, math.log(18.432), math.log(73.728))), 18.432, 73.728)
    expert_in = normal_values(key_list[20], (EXPERTS, D, 2 * FF), D ** -0.5, 0.1875, ((0, 4), (1, 8)), jnp.float32)
    in_first = normal_values(key_list[21], (EXPERTS, D, 2 * FF), (0.033 * (2 * TOKENS // EXPERTS) ** 0.5), 12.0, ((0, 4), (1, 8)), jnp.float32)
    in_second = jnp.clip(jnp.exp(math.log(1.47456) - 1.3862944 * jax.random.uniform(key_list[22], (EXPERTS, D, 2 * FF), jnp.float32) ** block_levels(key_list[22], (EXPERTS, D, 2 * FF), ((0, 4), (1, 8)), -0.2, 0.2)), 0.36864, 1.47456)
    expert_out = normal_values(key_list[23], (EXPERTS, FF, D), FF ** -0.5, 0.109375, ((0, 4), (1, 8)), jnp.float32)
    down_first = normal_values(key_list[24], (EXPERTS, FF, D), (0.0275 * (2 * TOKENS // EXPERTS) ** 0.5), 10.0, ((0, 4), (1, 8)), jnp.float32)
    down_second = jnp.clip(jnp.exp(math.log(1.024) - 1.3862944 * jax.random.uniform(key_list[25], (EXPERTS, FF, D), jnp.float32) ** block_levels(key_list[25], (EXPERTS, FF, D), ((0, 4), (1, 8)), -0.2, 0.2)), 0.256, 1.024)
    return {"tokens": tokens, "cotangent": cotangent, "seq_lengths": seq_lengths, "deal": deal, "routes": routes, "attn_qkv": attn_qkv, "qkv_first": qkv_first, "qkv_second": qkv_second, "attn_out": attn_out, "out_first": out_first, "out_second": out_second, "rel_bias": rel_bias, "bias_first": bias_first, "bias_second": bias_second, "router": router, "router_first": router_first, "router_second": router_second, "norm_gains": norm_gains, "gains_first": gains_first, "gains_second": gains_second, "expert_in": expert_in, "in_first": in_first, "in_second": in_second, "expert_out": expert_out, "down_first": down_first, "down_second": down_second}


@jax.custom_vjp
def low(v):
    return lax.optimization_barrier(v.astype(jnp.bfloat16)).astype(jnp.float32)

@jax.custom_vjp
def low_back(v):
    return v

def low_keep(v):
    return (low(v), None)

def low_pass(kept, grad):
    return (grad,)

def back_keep(v):
    return (v, None)

def back_low(kept, grad):
    return (low(grad),)
low.defvjp(low_keep, low_pass)
low_back.defvjp(back_keep, back_low)
highest = lax.Precision.HIGHEST
eps_norm = 1e-06
thresholds = (1, 2, 3, 4, 5, 6, 7, 8, 11, 16, 22, 32, 45, 64, 90)
beta_one = 0.9
beta_two = 0.999
eps_adam = 1e-08

def bucket_onehot(length):
    places = jnp.arange(length, dtype=jnp.int32)
    offset = places[None, :] - places[:, None]
    distance = jnp.abs(offset)
    bucket = 16 * (offset > 0).astype(jnp.int32)
    for threshold in thresholds:
        bucket = bucket + (distance >= threshold).astype(jnp.int32)
    return (bucket[:, :, None] == jnp.arange(BUCKETS, dtype=jnp.int32)[None, None, :]).astype(jnp.float32)

def adamw_update(weight, moment, second, gradient, step_rate, decay_factor):
    new_moment = beta_one * moment + (1.0 - beta_one) * gradient
    new_second = beta_two * second + (1.0 - beta_two) * gradient * gradient
    corrected = new_moment / (1.0 - beta_one ** STEP)
    scaled = new_second / (1.0 - beta_two ** STEP)
    new_weight = weight - step_rate * (corrected / (jnp.sqrt(scaled) + eps_adam) + decay_factor * weight)
    return (new_moment, new_second, new_weight)

def attend_one(x_rows, seq_length, gain_one, qkv_low, out_low, bias_table, onehot):
    scale_one = lax.rsqrt(lax.optimization_barrier(jnp.mean(x_rows * x_rows, axis=-1, keepdims=True)) + eps_norm)
    normed = low(x_rows * scale_one * gain_one)
    qkv = low(low_back(jnp.dot(normed, qkv_low, precision=highest)))
    queries = qkv[:, :D].reshape(TOK_DEV, HEADS, HEAD_DIM)
    key_rows = qkv[:, D:2 * D].reshape(TOK_DEV, HEADS, HEAD_DIM)
    values = qkv[:, 2 * D:].reshape(TOK_DEV, HEADS, HEAD_DIM)
    raw = jnp.einsum('ihd,jhd->hij', queries, key_rows, precision=highest) * (1.0 / math.sqrt(HEAD_DIM))
    raw = low_back(raw + jnp.einsum('ijb,bh->hij', onehot, bias_table, precision=highest))
    key_ok = jnp.arange(TOK_DEV, dtype=jnp.int32) < seq_length
    scores = jnp.where(key_ok[None, None, :], raw, -1e+30)
    weights = low(jax.nn.softmax(scores, axis=-1))
    context = jnp.einsum('hij,jhd->ihd', weights, values, precision=highest).reshape(TOK_DEV, D)
    context = low(low_back(context))
    return x_rows + low_back(jnp.dot(context, out_low, precision=highest))

def reference(tokens, cotangent, seq_lengths, deal, routes, attn_qkv, qkv_first, qkv_second, attn_out, out_first, out_second, rel_bias, bias_first, bias_second, router, router_first, router_second, norm_gains, gains_first, gains_second, expert_in, in_first, in_second, expert_out, down_first, down_second):
    group_size = math.gcd(NSEQ, max(1, 4096 // TOK_DEV))
    onehot = bucket_onehot(TOK_DEV)
    token_ids = jnp.arange(2 * TOKENS, dtype=jnp.int32) // 2
    flat_routes = routes.reshape(-1).astype(jnp.int32)
    route_hot = (routes.reshape(NSEQ, 2 * TOK_DEV)[:, :, None] == jnp.arange(EXPERTS, dtype=jnp.int32)[None, None, :]).astype(jnp.int32)
    before = jnp.cumsum(route_hot, axis=1) - route_hot
    slot_index = lax.optimization_barrier(jnp.sum(before * route_hot, axis=-1)).reshape(-1)
    target = token_ids // TOK_DEV * CAP + slot_index
    table = jnp.full((EXPERTS, NSEQ * CAP), TOKENS, jnp.int32).at[flat_routes, target].set(token_ids)
    places = jnp.arange(TOKENS, dtype=jnp.int32)
    valid_rows = (places % TOK_DEV < seq_lengths[places // TOK_DEV]).astype(jnp.float32)
    chosen = (routes[:, :, None] == jnp.arange(EXPERTS, dtype=jnp.int32)[None, None, :]).astype(jnp.float32)
    deal_index = deal.astype(jnp.int32)

    def forward(x_float, qkv_weight, out_weight, bias_table, router_weight, gain_weight, in_weight, down_weight):
        gain_one = gain_weight[:, 0]
        gain_two = gain_weight[:, 1]
        qkv_low = low(qkv_weight)
        out_low = low(out_weight)
        in_low = low(in_weight)
        down_low = low(down_weight)

        def attend(seq_block):
            row_block, len_block = seq_block
            return jax.vmap(lambda one_rows, one_len: attend_one(one_rows, one_len, gain_one, qkv_low, out_low, bias_table, onehot))(row_block, len_block)
        hidden_one = lax.map(jax.checkpoint(attend), (x_float.reshape(NSEQ // group_size, group_size, TOK_DEV, D), seq_lengths.reshape(NSEQ // group_size, group_size))).reshape(TOKENS, D)
        scale_two = lax.rsqrt(lax.optimization_barrier(jnp.mean(hidden_one * hidden_one, axis=-1, keepdims=True)) + eps_norm)
        normed = low(hidden_one * scale_two * gain_two)
        router_probs = jax.nn.softmax(jnp.dot(normed, router_weight, precision=highest), axis=-1)
        picked = lax.optimization_barrier(jnp.sum(router_probs[:, None, :] * chosen, axis=-1))
        gate_value = picked / lax.optimization_barrier(jnp.sum(picked, axis=-1, keepdims=True))
        combine = gate_value * valid_rows[:, None]
        padded = jnp.concatenate([normed, jnp.zeros((1, D), jnp.float32)], axis=0)

        def expert_one(expert_item):
            table_row, in_one, down_one = expert_item
            rows_in = padded[table_row]
            projected = low_back(jnp.dot(rows_in, in_one, precision=highest))
            active = low(jax.nn.gelu(projected[:, :FF], approximate=True) * projected[:, FF:])
            return low(low_back(jnp.dot(active, down_one, precision=highest)))
        outputs = lax.map(jax.checkpoint(expert_one), (table, in_low, down_low))
        gathered = outputs[flat_routes, target].reshape(TOKENS, 2, D)
        mixture = lax.optimization_barrier(jnp.sum(combine[:, :, None] * gathered, axis=1))
        return valid_rows[:, None] * (hidden_one + mixture)
    result, pullback = jax.vjp(forward, tokens.astype(jnp.float32), attn_qkv, attn_out, rel_bias, router, norm_gains, expert_in, expert_out)
    loader_cot = cotangent.astype(jnp.float32).reshape(NSEQ, TOK_DEV, D)[deal_index].reshape(TOKENS, D)
    grads = pullback(loader_cot)
    dealt_out = jnp.zeros((NSEQ, TOK_DEV, D), jnp.float32).at[deal_index].set(result.reshape(NSEQ, TOK_DEV, D)).reshape(TOKENS, D)
    qkv_new = adamw_update(attn_qkv, qkv_first, qkv_second, grads[1], 1.5 / math.sqrt(D), 0.1)
    out_new = adamw_update(attn_out, out_first, out_second, grads[2], 6.0 / math.sqrt(D), 0.1)
    bias_new = adamw_update(rel_bias, bias_first, bias_second, grads[3], 0.3, 0.0)
    router_new = adamw_update(router, router_first, router_second, grads[4], 1.0 / math.sqrt(D), 0.1)
    gains_new = adamw_update(norm_gains, gains_first, gains_second, grads[5], 0.5, 0.0)
    in_new = adamw_update(expert_in, in_first, in_second, grads[6], 1.5 / math.sqrt(D), 0.1)
    down_new = adamw_update(expert_out, down_first, down_second, grads[7], 1.5 / math.sqrt(FF), 0.1)
    return (dealt_out.astype(jnp.bfloat16), grads[0], qkv_new[0], qkv_new[1], qkv_new[2], out_new[0], out_new[1], out_new[2], bias_new[0], bias_new[1], bias_new[2], router_new[0], router_new[1], router_new[2], gains_new[0], gains_new[1], gains_new[2], in_new[0], in_new[1], in_new[2], down_new[0], down_new[1], down_new[2])
```

```python
import math

import jax
import jax.numpy as jnp
from jax import lax
from jax.sharding import Mesh
from jax.sharding import PartitionSpec as P

D = 1024
HEADS = 16
FF = 2816
BUCKETS = 32
STEP = 10
QUAD = 4
REP = ("grp", "quad")
PLANE = ("quad", "exp")
ALL = ("grp", "quad", "exp")

highest = lax.Precision.HIGHEST
eps_norm = 1e-06
thresholds = (1, 2, 3, 4, 5, 6, 7, 8, 11, 16, 22, 32, 45, 64, 90)
beta_one = 0.9
beta_two = 0.999
eps_adam = 1e-08
low = jnp.bfloat16
full = jnp.float32


def bucket_onehot(length):
    places = jnp.arange(length, dtype=jnp.int32)
    offset = places[None, :] - places[:, None]
    distance = jnp.abs(offset)
    bucket = 16 * (offset > 0).astype(jnp.int32)
    for threshold in thresholds:
        bucket = bucket + (distance >= threshold).astype(jnp.int32)
    return (bucket[:, :, None] == jnp.arange(BUCKETS, dtype=jnp.int32)[None, None, :]).astype(full)


def adamw_update(weight, moment, second, gradient, step_rate, decay_factor):
    new_moment = beta_one * moment + (1.0 - beta_one) * gradient
    new_second = beta_two * second + (1.0 - beta_two) * gradient * gradient
    corrected = new_moment / (1.0 - beta_one**STEP)
    scaled = new_second / (1.0 - beta_two**STEP)
    new_weight = weight - step_rate * (
        corrected / (jnp.sqrt(scaled) + eps_adam) + decay_factor * weight
    )
    return (new_moment, new_second, new_weight)


def gated_unit(gate_input, up_input):
    return jax.nn.gelu(gate_input, approximate=True) * up_input


def dot(a, b):
    return jnp.dot(a, b, preferred_element_type=full)


def swap(pieces, axes):
    return lax.all_to_all(pieces, axes, split_axis=0, concat_axis=0, tiled=True)


def spread(block, axes):
    members = lax.axis_size(axes)
    return swap(jnp.broadcast_to(block[None], (members,) + block.shape), axes)


def per_device(
    tokens,
    cotangent,
    seq_lengths,
    deal,
    routes,
    attn_qkv,
    qkv_first,
    qkv_second,
    attn_out,
    out_first,
    out_second,
    rel_bias,
    bias_first,
    bias_second,
    router,
    router_first,
    router_second,
    norm_gains,
    gains_first,
    gains_second,
    expert_in,
    in_first,
    in_second,
    expert_out,
    down_first,
    down_second,
):
    rows, width = tokens.shape
    head_dim = width // HEADS
    score_scale = 1.0 / math.sqrt(head_dim)
    experts = router.shape[1]
    capacity = (10 * rows + 4 * experts - 1) // (4 * experts)
    exps = lax.axis_size("exp")
    grps = lax.axis_size("grp")
    reps = grps * QUAD
    heads = HEADS // exps
    head_cols = heads * head_dim
    place = lax.axis_index("exp")
    base = lax.axis_index(REP) * exps
    me = base + place
    slab = expert_in.shape[1]
    units = expert_out.shape[1]
    quarter = grps * units

    row_block = attn_qkv.shape[0]
    qkv_rows = lax.all_gather(attn_qkv.astype(low), REP, axis=1, tiled=True)
    out_rows = lax.all_gather(attn_out.astype(low), REP, axis=1, tiled=True)
    qkv_pieces = jnp.transpose(
        qkv_rows.reshape(row_block, 3, exps, head_cols), (2, 0, 1, 3)
    ).reshape(exps, row_block, 3 * head_cols)
    qkv_mine = swap(qkv_pieces, "exp").reshape(width, 3 * head_cols)
    full_out = spread(out_rows, "exp").reshape(width, width)

    group_tokens = spread(tokens, "exp")
    group_cotangent = spread(cotangent, "exp")
    my_cotangent = lax.dynamic_index_in_dim(group_cotangent, deal[me] - base, 0, keepdims=False)

    my_routes = lax.dynamic_slice_in_dim(routes, me * rows, rows, 0)
    places = jnp.arange(rows, dtype=jnp.int32)
    valid_rows = (places < seq_lengths[me]).astype(full)
    group_lengths = lax.dynamic_slice_in_dim(seq_lengths, base, exps, 0)
    key_ok = places[None, :] < group_lengths[:, None]
    gain_one = norm_gains[:, 0]
    gain_two = norm_gains[:, 1]

    chosen = (my_routes[:, :, None] == jnp.arange(experts, dtype=jnp.int32)[None, None, :]).astype(full)
    flat_routes = my_routes.reshape(-1)
    route_hot = (flat_routes[:, None] == jnp.arange(experts, dtype=jnp.int32)[None, :]).astype(jnp.int32)
    before = jnp.cumsum(route_hot, axis=0) - route_hot
    slot_index = jnp.sum(before * route_hot, axis=-1)
    target = (flat_routes * capacity + slot_index).reshape(rows, 2)
    slots = experts * capacity
    slot_ids = jnp.arange(slots, dtype=jnp.int32)
    place_first = slot_ids[:, None] == target[None, :, 0]
    place_second = slot_ids[:, None] == target[None, :, 1]
    place_any = jnp.logical_or(place_first, place_second).astype(low)

    shard_in = expert_in[0].astype(low).reshape(slab, 2, grps, QUAD, units)
    in_pieces = jnp.transpose(shard_in, (1, 3, 0, 2, 4)).reshape(2, 1, QUAD, slab, quarter)
    in_pieces = jnp.broadcast_to(in_pieces, (2, grps, QUAD, slab, quarter)).reshape(
        2, reps, slab, quarter
    )
    down_mine = spread(expert_out[0].astype(low), "grp").reshape(quarter, width)
    gate_mine = swap(in_pieces[0], REP).reshape(width, quarter)
    up_mine = swap(in_pieces[1], REP).reshape(width, quarter)

    upstream = my_cotangent.astype(full) * valid_rows[:, None]

    def to_experts(block):
        sent = block.reshape((1, experts) + block.shape[1:])
        sent = jnp.broadcast_to(sent, (QUAD,) + sent.shape[1:])
        return swap(sent.reshape((QUAD * experts,) + block.shape[1:]), PLANE)

    def dispatch(values):
        return dot(place_any, values).astype(low).reshape(experts, capacity, width)

    expert_upstream = to_experts(dispatch(upstream.astype(low))).reshape(-1, width)
    active_grad_bare = lax.dot_general(
        expert_upstream, down_mine, (((1,), (1,)), ((), ())), preferred_element_type=full
    )

    x_group = group_tokens.astype(full)
    scale_group = lax.rsqrt(jnp.mean(x_group * x_group, axis=-1, keepdims=True) + eps_norm)
    normed_group = (x_group * scale_group * gain_one).astype(low).reshape(exps * rows, width)
    qkv = dot(normed_group, qkv_mine).astype(low).reshape(exps, rows, 3, heads, head_dim)
    queries = qkv[:, :, 0]
    key_rows = qkv[:, :, 1]
    values = qkv[:, :, 2]
    onehot = bucket_onehot(rows)
    bias_mine = lax.dynamic_slice_in_dim(rel_bias, place * heads, heads, 1)
    bias_table = jnp.einsum("ijb,bh->hij", onehot, bias_mine, precision=highest)

    def scores_of():
        raw = (
            jnp.einsum("sihd,sjhd->shij", queries, key_rows, preferred_element_type=full)
            * score_scale
            + bias_table[None]
        )
        return jnp.where(key_ok[:, None, None, :], raw, -1e30)

    scores = scores_of()
    row_max = jnp.max(scores, axis=-1, keepdims=True)
    log_total = row_max + jnp.log(jnp.sum(jnp.exp(scores - row_max), axis=-1, keepdims=True))
    weights_low = jnp.exp(scores - log_total).astype(low)
    context_mine = (
        jnp.einsum("shij,sjhd->sihd", weights_low, values, preferred_element_type=full)
        .astype(low)
        .reshape(exps, rows, head_cols)
    )
    context = jnp.transpose(swap(context_mine, "exp"), (1, 0, 2)).reshape(rows, width)

    x_float = tokens.astype(full)
    scale_one = lax.rsqrt(jnp.mean(x_float * x_float, axis=-1, keepdims=True) + eps_norm)
    hidden_one = x_float + dot(context, full_out)
    scale_two = lax.rsqrt(jnp.mean(hidden_one * hidden_one, axis=-1, keepdims=True) + eps_norm)
    normed_two = (hidden_one * scale_two * gain_two).astype(low)
    normed_float = normed_two.astype(full)
    router_probs = jax.nn.softmax(jnp.dot(normed_float, router, precision=highest), axis=-1)
    picked = jnp.sum(router_probs[:, None, :] * chosen, axis=-1)
    gate_total = jnp.sum(picked, axis=-1, keepdims=True)
    gate_value = picked / gate_total
    combine = gate_value * valid_rows[:, None]
    combine_slots = jnp.sum(
        jnp.where(place_first, combine[None, :, 0], 0.0)
        + jnp.where(place_second, combine[None, :, 1], 0.0),
        axis=1,
    ).reshape(experts, 1, capacity)

    expert_rows = to_experts(dispatch(normed_two)).reshape(-1, width)
    expert_combine = to_experts(combine_slots).reshape(-1, 1)

    gate_part = dot(expert_rows, gate_mine)
    up_part = dot(expert_rows, up_mine)
    active_float, active_pull = jax.vjp(gated_unit, gate_part, up_part)
    active = active_float.astype(low)
    active_scaled = (active_float * expert_combine).astype(low)
    combine_grad_part = jnp.sum(active_float * active_grad_bare, axis=-1).reshape(
        QUAD * experts, 1, capacity
    )
    gate_part_grad, up_part_grad = active_pull(active_grad_bare * expert_combine)
    gate_part_grad = gate_part_grad.astype(low)
    up_part_grad = up_part_grad.astype(low)
    rows_grad_part = (
        lax.dot_general(gate_part_grad, gate_mine, (((1,), (1,)), ((), ())), preferred_element_type=full)
        + lax.dot_general(up_part_grad, up_mine, (((1,), (1,)), ((), ())), preferred_element_type=full)
    ).astype(low)
    output_part = dot(active, down_mine).astype(low)

    combine_grad_back = swap(combine_grad_part, PLANE)
    rows_grad_back = swap(rows_grad_part.reshape(QUAD * experts, capacity, width), PLANE)
    output_back = swap(output_part.reshape(QUAD * experts, capacity, width), PLANE)

    def transposed_dot(a, b):
        return lax.dot_general(a, b, (((0,), (0,)), ((), ())), preferred_element_type=full)

    down_grad = transposed_dot(active_scaled, expert_upstream).astype(low)
    gate_grad = transposed_dot(expert_rows, gate_part_grad).astype(low)
    up_grad = transposed_dot(expert_rows, up_part_grad).astype(low)
    down_share = jnp.sum(
        swap(down_grad.reshape(grps, units, width), "grp").astype(full), axis=0
    )[None]

    def in_columns(grad):
        back = swap(grad.reshape(reps, slab, quarter), REP).astype(full)
        back = jnp.sum(back.reshape(grps, QUAD, slab, grps, units), axis=0)
        return jnp.transpose(back, (1, 2, 0, 3)).reshape(slab, grps * QUAD * units)

    in_share = jnp.concatenate([in_columns(gate_grad), in_columns(up_grad)], axis=1)[None]

    def from_slots(placed, parts):
        hot = jnp.broadcast_to(placed.astype(low)[None], (QUAD,) + placed.shape).reshape(-1, rows)
        return lax.dot_general(
            hot, parts.reshape(-1, width), (((0,), (0,)), ((), ())), preferred_element_type=full
        )

    mixture = combine[:, :1] * from_slots(place_first, output_back) + combine[:, 1:] * from_slots(
        place_second, output_back
    )
    block_loader = (valid_rows[:, None] * (hidden_one + mixture)).astype(low)
    seq_ids = jnp.arange(deal.shape[0], dtype=jnp.int32)
    dealt_seq = jnp.sum(jnp.where(deal == me, seq_ids, 0))
    block_out = lax.dynamic_index_in_dim(
        spread(block_loader, "exp"), dealt_seq - base, 0, keepdims=False
    )

    combine_grad_slots = jnp.sum(combine_grad_back.reshape(QUAD, slots), axis=0)
    combine_grad = jnp.stack(
        [
            jnp.sum(jnp.where(place_first, combine_grad_slots[:, None], 0.0), axis=0),
            jnp.sum(jnp.where(place_second, combine_grad_slots[:, None], 0.0), axis=0),
        ],
        axis=1,
    )
    gate_grad_value = combine_grad * valid_rows[:, None]
    picked_grad = (
        gate_grad_value - jnp.sum(gate_grad_value * gate_value, axis=-1, keepdims=True)
    ) / gate_total
    probs_grad = jnp.sum(picked_grad[:, :, None] * chosen, axis=1)
    logit_grad = router_probs * (
        probs_grad - jnp.sum(probs_grad * router_probs, axis=-1, keepdims=True)
    )
    router_grad = jnp.dot(normed_float.T, logit_grad, precision=highest)
    normed_grad = jnp.dot(logit_grad, router.T, precision=highest) + from_slots(
        jnp.logical_or(place_first, place_second), rows_grad_back
    )
    scaled_two = normed_grad * gain_two
    hidden_grad = (
        upstream
        + scale_two * scaled_two
        - hidden_one * scale_two**3 * jnp.mean(scaled_two * hidden_one, axis=-1, keepdims=True)
    )
    gain_two_grad = jnp.sum(normed_grad * hidden_one * scale_two, axis=0)
    branch_grad = hidden_grad.astype(low)
    context_grad = lax.dot_general(
        branch_grad, full_out, (((1,), (1,)), ((), ())), preferred_element_type=full
    ).astype(low)
    context_grad_pieces = jnp.transpose(context_grad.reshape(rows, exps, head_cols), (1, 0, 2))
    context_grad_mine = swap(context_grad_pieces, "exp").reshape(exps, rows, heads, head_dim)
    branch_group = spread(branch_grad, "exp").reshape(exps * rows, width)
    out_grad = transposed_dot(context_mine.reshape(exps * rows, head_cols), branch_group).astype(low)

    scores = scores_of()
    probs_again = jnp.exp(scores - log_total)
    weights_again = probs_again.astype(low)
    values_grad = jnp.einsum(
        "shij,sihd->sjhd", weights_again, context_grad_mine, preferred_element_type=full
    )
    probs_grad_att = jnp.einsum(
        "sihd,sjhd->shij", context_grad_mine, values, preferred_element_type=full
    )
    row_delta = jnp.sum(probs_grad_att * probs_again, axis=-1, keepdims=True)
    scores_grad = (probs_again * (probs_grad_att - row_delta)).astype(low)
    scores_grad_sum = jnp.sum(scores_grad.astype(full), axis=0)
    bias_grad_mine = jnp.einsum("hij,ijb->bh", scores_grad_sum, onehot, precision=highest)
    bias_grad = lax.dynamic_update_slice_in_dim(
        jnp.zeros((BUCKETS, HEADS), full), bias_grad_mine, place * heads, 1
    )
    queries_grad = (
        jnp.einsum("shij,sjhd->sihd", scores_grad, key_rows, preferred_element_type=full)
        * score_scale
    )
    keys_grad = (
        jnp.einsum("shij,sihd->sjhd", scores_grad, queries, preferred_element_type=full)
        * score_scale
    )
    qkv_grad = (
        jnp.stack([queries_grad, keys_grad, values_grad], axis=2)
        .astype(low)
        .reshape(exps * rows, 3 * head_cols)
    )
    normed_one_part = lax.dot_general(
        qkv_grad, qkv_mine, (((1,), (1,)), ((), ())), preferred_element_type=full
    ).astype(low)
    normed_one_grad = jnp.sum(
        swap(normed_one_part.reshape(exps, rows, width), "exp").astype(full), axis=0
    )
    scaled_one = normed_one_grad * gain_one
    token_grad = (
        hidden_grad
        + scale_one * scaled_one
        - x_float * scale_one**3 * jnp.mean(scaled_one * x_float, axis=-1, keepdims=True)
    )
    gain_one_grad = jnp.sum(normed_one_grad * x_float * scale_one, axis=0)

    qkv_weight_grad = transposed_dot(normed_group, qkv_grad).astype(low)
    qkv_grad_rows = swap(qkv_weight_grad.reshape(exps, row_block, 3 * head_cols), "exp")
    qkv_grad_rows = jnp.transpose(
        qkv_grad_rows.reshape(exps, row_block, 3, head_cols), (1, 2, 0, 3)
    ).reshape(row_block, reps, -1)
    qkv_share = jnp.sum(
        swap(jnp.transpose(qkv_grad_rows, (1, 0, 2)), REP).astype(full), axis=0
    )
    out_pieces = jnp.transpose(out_grad.reshape(row_block, reps, -1), (1, 0, 2))
    out_share = jnp.sum(swap(out_pieces, REP).astype(full), axis=0)

    small = jnp.concatenate(
        [
            router_grad.reshape(-1),
            jnp.stack([gain_one_grad, gain_two_grad], axis=1).reshape(-1),
            bias_grad.reshape(-1),
        ]
    ).reshape(-1, 128)
    small_total = jnp.sum(lax.all_gather(small, ALL, axis=0, tiled=False), axis=0).reshape(-1)
    router_total = small_total[: router.size].reshape(router.shape)
    gains_total = small_total[router.size : router.size + norm_gains.size].reshape(norm_gains.shape)
    bias_total = small_total[router.size + norm_gains.size :].reshape(rel_bias.shape)

    qkv_new = adamw_update(attn_qkv, qkv_first, qkv_second, qkv_share, 1.5 / math.sqrt(D), 0.1)
    out_new = adamw_update(attn_out, out_first, out_second, out_share, 6.0 / math.sqrt(D), 0.1)
    bias_new = adamw_update(rel_bias, bias_first, bias_second, bias_total, 0.3, 0.0)
    router_new = adamw_update(
        router, router_first, router_second, router_total, 1.0 / math.sqrt(D), 0.1
    )
    gains_new = adamw_update(norm_gains, gains_first, gains_second, gains_total, 0.5, 0.0)
    in_new = adamw_update(expert_in, in_first, in_second, in_share, 1.5 / math.sqrt(D), 0.1)
    down_new = adamw_update(
        expert_out, down_first, down_second, down_share, 1.5 / math.sqrt(FF), 0.1
    )
    return (
        (block_out, token_grad)
        + qkv_new
        + out_new
        + bias_new
        + router_new
        + gains_new
        + in_new
        + down_new
    )


def solution(mesh):
    reps, exps = mesh.devices.shape
    split = Mesh(mesh.devices.reshape(reps // QUAD, QUAD, exps), ALL)
    by_rows = P(ALL, None)
    attn = P("exp", REP)
    expert = P("exp", REP, None)
    return jax.shard_map(
        per_device,
        mesh=split,
        in_specs=(by_rows, by_rows) + (P(),) * 3 + (attn,) * 6 + (P(),) * 9 + (expert,) * 6,
        out_specs=(by_rows, by_rows) + (attn,) * 6 + (P(),) * 9 + (expert,) * 6,
        check_vma=False,
    )
```

```python
import functools
import math

import jax
import jax.numpy as jnp
from jax import lax
from jax.experimental import pallas as pl
from jax.experimental.pallas import tpu as pltpu
from jax.sharding import Mesh
from jax.sharding import PartitionSpec as P

D = 1024
HEADS = 16
FF = 2816
BUCKETS = 32
STEP = 10
QUAD = 4
REP = ("grp", "quad")
PLANE = ("quad", "exp")
ALL = ("grp", "quad", "exp")

highest = lax.Precision.HIGHEST
eps_norm = 1e-06
thresholds = (1, 2, 3, 4, 5, 6, 7, 8, 11, 16, 22, 32, 45, 64, 90)
beta_one = 0.9
beta_two = 0.999
eps_adam = 1e-08
low = jnp.bfloat16
full = jnp.float32
MESH = pl.DeviceIdType.MESH


def bucket_onehot(length):
    places = jnp.arange(length, dtype=jnp.int32)
    offset = places[None, :] - places[:, None]
    distance = jnp.abs(offset)
    bucket = 16 * (offset > 0).astype(jnp.int32)
    for threshold in thresholds:
        bucket = bucket + (distance >= threshold).astype(jnp.int32)
    return (bucket[:, :, None] == jnp.arange(BUCKETS, dtype=jnp.int32)[None, None, :]).astype(full)


def adamw_update(weight, moment, second, gradient, step_rate, decay_factor):
    new_moment = beta_one * moment + (1.0 - beta_one) * gradient
    new_second = beta_two * second + (1.0 - beta_two) * gradient * gradient
    corrected = new_moment / (1.0 - beta_one**STEP)
    scaled = new_second / (1.0 - beta_two**STEP)
    new_weight = weight - step_rate * (
        corrected / (jnp.sqrt(scaled) + eps_adam) + decay_factor * weight
    )
    return (new_moment, new_second, new_weight)


def gated_unit(gate_input, up_input):
    return jax.nn.gelu(gate_input, approximate=True) * up_input


def dot(a, b):
    return jnp.dot(a, b, preferred_element_type=full)


def swap(pieces, axes):
    return lax.all_to_all(pieces, axes, split_axis=0, concat_axis=0, tiled=True)


def spread(block, axes):
    members = lax.axis_size(axes)
    return swap(jnp.broadcast_to(block[None], (members,) + block.shape), axes)


def nt(a, b, precision=None):
    return lax.dot_general(a, b, (((1,), (1,)), ((), ())), preferred_element_type=full, precision=precision)


def tn(a, b):
    return lax.dot_general(a, b, (((0,), (0,)), ((), ())), preferred_element_type=full)


class Where:
    def __init__(self, grps, exps):
        self.grps, self.exps = grps, exps
        self.reps = grps * QUAD
        self.grp = lax.axis_index("grp")
        self.quad = lax.axis_index("quad")
        self.exp = lax.axis_index("exp")
        self.rep = self.grp * QUAD + self.quad
        self.base = self.rep * exps
        self.me = self.base + self.exp

    def device(self, rep, exp):
        return (rep // QUAD, rep % QUAD, exp)

    def near(self, flip):
        q = self.quad
        if flip & 1:
            q = q + 1 - 2 * (q % 2)
        if flip & 2:
            q = q + 2 - 4 * (q // 2)
        return q


def send(src, dst, send_sem, recv_sem, device):
    return pltpu.make_async_remote_copy(
        src_ref=src, dst_ref=dst, send_sem=send_sem, recv_sem=recv_sem, device_id=device, device_id_type=MESH
    )


def arrived(ref, sem):
    pltpu.make_async_copy(ref, ref, sem).wait()


def greet_all(at):
    count = at.reps * at.exps
    barrier = pltpu.get_barrier_semaphore()

    def greet(k, _):
        other = (at.me + k) % count
        pl.semaphore_signal(
            barrier, inc=1, device_id=at.device(other // at.exps, other % at.exps), device_id_type=MESH
        )
        return 0

    lax.fori_loop(1, count, greet, 0)
    pl.semaphore_wait(barrier, count - 1)


def lane_of(shape):
    return lax.broadcasted_iota(jnp.int32, shape, 1)


def row_of(shape):
    return lax.broadcasted_iota(jnp.int32, shape, 0)


def bucket_of(offset):
    distance = jnp.abs(offset)
    bucket = jnp.where(offset > 0, 16, 0)
    for threshold in thresholds:
        bucket = bucket + jnp.where(distance >= threshold, 1, 0)
    return bucket


def forward_kernel(
    grps,
    exps,
    cap,
    lengths,
    deal,
    rel_bias,
    routes_row,
    routes_col,
    tokens,
    cotangent,
    gains,
    router,
    qkv_t,
    out_w,
    gate_pieces,
    up_pieces,
    down_slab,
    gate_w,
    up_w,
    down_w,
    g_rows,
    n_rows,
    comb_rows,
    qkv_out,
    lse_out,
    mine_out,
    n1_out,
    wqkv_out,
    wout_out,
    h1_out,
    n2_out,
    g_out,
    probs_out,
    comb_out,
    place_out,
    tok_all,
    cot_all,
    wqkv,
    wout,
    n1,
    qkv,
    lse,
    mine,
    ctx,
    bias,
    place,
    g_send,
    n_send,
    comb_send,
    tok_sem,
    cot_sem,
    wq_sem,
    wo_sem,
    wo2_sem,
    weight_sem,
    weight2_sem,
    ctx_sem,
    row_sem,
    hop_sem,
    store_sem,
):
    at = Where(grps, exps)
    reps = at.reps
    rows, width = tokens.shape
    heads = HEADS // exps
    head_dim = width // HEADS
    head_cols = heads * head_dim
    block_cols = min(128, head_cols)
    shard_cols, row_block = qkv_t.shape
    seg = math.gcd(shard_cols, head_cols)
    segs = shard_cols // seg
    slab = gate_pieces.shape[1]
    scale = 1.0 / math.sqrt(head_dim)
    SEND, RECV = 0, 1

    greet_all(at)

    def exp_peer(k):
        return (at.exp + k) % exps

    for k in range(1, exps):
        peer = exp_peer(k)
        send(
            tokens, tok_all.at[at.exp], tok_sem.at[SEND, peer], tok_sem.at[RECV, at.exp], at.device(at.rep, peer)
        ).start()
    tok_all[at.exp] = tokens[...]

    def segment(k):
        col = (at.rep * segs + k) * seg
        section = col // width
        within = col - section * width
        owner = within // head_cols
        return owner, section * head_cols + within - owner * head_cols

    def segment_copy(k, shift):
        owner, offset = segment(k)
        src = qkv_t.at[pl.ds(k * seg, seg)]
        dst = wqkv.at[at.exp, pl.ds(pl.multiple_of(offset, seg), seg)]
        target = at.device((at.rep + shift) % reps, owner)
        return owner, src, dst, send(
            src, dst, wq_sem.at[SEND, k * reps + shift], wq_sem.at[RECV, at.exp * 3 * (head_cols // seg) + offset // seg], target
        )

    def over_segments(act, act_local):
        def one(i, _):
            k, shift = i // reps, i % reps
            owner, src, dst, copy = segment_copy(k, shift)
            stays = jnp.logical_and(shift == 0, owner == at.exp)

            @pl.when(jnp.logical_not(stays))
            def _():
                act(copy)

            @pl.when(stays)
            def _():
                act_local(k, src, dst)

            return 0

        lax.fori_loop(0, segs * reps, one, 0)

    def local_segment(k, src, dst):
        _, offset = segment(k)
        pltpu.make_async_copy(src, dst, wq_sem.at[RECV, at.exp * 3 * (head_cols // seg) + offset // seg]).start()

    over_segments(lambda copy: copy.start(), local_segment)

    for k in range(1, reps):
        other = (at.rep + k) % reps
        send(
            out_w, wout.at[at.exp, at.rep], wo_sem.at[SEND, other], wo_sem.at[RECV, at.rep], at.device(other, at.exp)
        ).start()
    wout[at.exp, at.rep] = out_w[...]
    for k in range(1, exps):
        peer = exp_peer(k)
        send(
            cotangent, cot_all.at[at.exp], cot_sem.at[SEND, peer], cot_sem.at[RECV, at.exp], at.device(at.rep, peer)
        ).start()
    cot_all[at.exp] = cotangent[...]

    span = 2 * rows
    bucket = bucket_of(lane_of((8, span)) - rows)
    for h in range(heads):
        line = jnp.zeros((8, span), full)
        for b in range(BUCKETS):
            line = jnp.where(bucket == b, rel_bias[b, at.exp * heads + h], line)
        whole = jnp.broadcast_to(line[0:1], (rows, span))
        bias[h] = pltpu.roll(whole, 0, 1, stride=1, stride_axis=0)[:, rows:]

    first, second = routes_row[0:1, :], routes_row[1:2, :]
    expert_row = row_of((max(8, exps), rows))
    hot = jnp.logical_or(expert_row == first, expert_row == second)
    hot_low = jnp.where(hot, 1.0, 0.0).astype(low)
    earlier = jnp.where(row_of((rows, rows)) < lane_of((rows, rows)), 1.0, 0.0).astype(low)
    before = jnp.dot(hot_low, earlier, preferred_element_type=full)
    slot = row_of((cap, rows)).astype(full)
    for e in range(exps):
        inside = jnp.logical_and(slot == before[e : e + 1, :], hot_low[e : e + 1, :].astype(full) > 0.5)
        place[e] = jnp.where(inside, 1.0, 0.0).astype(low)

    def norm_group(s, _):
        @pl.when(s != at.exp)
        def _():
            arrived(tok_all.at[s], tok_sem.at[RECV, s])

        x = tok_all[s].astype(full)
        r = lax.rsqrt(jnp.mean(x * x, axis=1, keepdims=True) + eps_norm)
        n1[s] = (x * r * gains[0:1, :]).astype(low)
        return 0

    lax.fori_loop(0, exps, norm_group, 0)

    def wait_segment(i, _):
        e, j = i // (3 * head_cols // seg), i % (3 * head_cols // seg)
        arrived(wqkv.at[e, pl.ds(pl.multiple_of(j * seg, seg), seg)], wq_sem.at[RECV, i])
        return 0

    lax.fori_loop(0, exps * 3 * head_cols // seg, wait_segment, 0)

    def weight_copies(k):
        other = (at.rep + k) % reps
        device = at.device(other, at.exp)
        here = pl.ds(pl.multiple_of(at.rep * slab, slab), slab)
        return [
            send(
                gate_pieces.at[other % QUAD], gate_w.at[here], weight_sem.at[SEND, other], weight_sem.at[RECV, at.rep], device
            ),
            send(
                up_pieces.at[other % QUAD], up_w.at[here], weight2_sem.at[SEND, other], weight2_sem.at[RECV, at.rep], device
            ),
        ]

    def own_weights():
        here = pl.ds(pl.multiple_of(at.rep * slab, slab), slab)
        return [
            pltpu.make_async_copy(gate_pieces.at[at.quad], gate_w.at[here], weight_sem.at[RECV, at.rep]),
            pltpu.make_async_copy(up_pieces.at[at.quad], up_w.at[here], weight2_sem.at[RECV, at.rep]),
            pltpu.make_async_copy(down_slab, down_w.at[at.grp], weight_sem.at[RECV, reps + at.grp]),
        ]

    def down_copies():
        return [
            send(
                down_slab,
                down_w.at[at.grp],
                weight_sem.at[SEND, reps + (at.grp + k) % grps],
                weight_sem.at[RECV, reps + at.grp],
                ((at.grp + k) % grps, at.quad, at.exp),
            )
            for k in range(1, grps)
        ]

    for copy in down_copies():
        copy.start()

    def start_weights(k, _):
        for copy in weight_copies(k):
            copy.start()
        return 0

    lax.fori_loop(1, reps, start_weights, 0)
    for copy in own_weights():
        copy.start()

    def project(s, _):
        total = jnp.zeros((rows, 3 * head_cols), full)
        for e in range(exps):
            total = total + nt(n1[s, :, e * row_block : (e + 1) * row_block], wqkv[e])
        qkv[s] = total.astype(low)
        return 0

    lax.fori_loop(0, exps, project, 0)

    for k in range(1, reps):
        other = (at.rep + k) % reps
        arrived(wout.at[at.exp, other], wo_sem.at[RECV, other])

    def wout_copies():
        return [
            send(
                wout.at[at.exp],
                wout.at[at.exp],
                wo2_sem.at[SEND, exp_peer(k)],
                wo2_sem.at[RECV, at.exp],
                at.device(at.rep, exp_peer(k)),
            )
            for k in range(1, exps)
        ]

    for copy in wout_copies():
        copy.start()

    for k in range(1, exps):
        peer = exp_peer(k)
        arrived(cot_all.at[peer], cot_sem.at[RECV, peer])
    mine_place = deal[at.me] - at.base
    g = jnp.zeros((rows, width), full)
    for e in range(exps):
        g = jnp.where(mine_place == e, cot_all[e].astype(full), g)
    valid = row_of((rows, 1)) < lengths[at.me]
    g = jnp.where(valid, g, 0.0).astype(low)
    g_out[...] = g

    def dispatch(values, into):
        def one(e, _):
            into[e] = jnp.dot(place[e], values, preferred_element_type=full).astype(low)
            return 0

        lax.fori_loop(0, exps, one, 0)

    def row_copies(source, dest, sems):
        return [
            send(
                source.at[exp_peer(k)],
                dest.at[at.quad, at.exp],
                row_sem.at[sems, SEND, exp_peer(k)],
                row_sem.at[sems, RECV, at.exp],
                at.device(at.rep, exp_peer(k)),
            )
            for k in range(1, exps)
        ]

    def own_row_copy(source, dest, sems):
        return pltpu.make_async_copy(source.at[at.exp], dest.at[at.quad, at.exp], row_sem.at[sems, RECV, at.exp])

    def row_starts(source, dest, sems):
        for copy in row_copies(source, dest, sems):
            copy.start()
        own_row_copy(source, dest, sems).start()

    def rows_in(dest, sems):
        for e in range(exps):
            arrived(dest.at[at.quad, e], row_sem.at[sems, RECV, e])

    def hops(dest, sems, one, two):
        def hop(block, flip, index):
            return send(
                dest.at[block],
                dest.at[block],
                hop_sem.at[sems, SEND, index],
                hop_sem.at[sems, RECV, index],
                (at.grp, at.near(flip), at.exp),
            )

        return [hop(at.quad, one, 0), hop(at.quad, two, 1), hop(at.near(one), two, 2)]

    def hop_in(dest, sems, index, block):
        arrived(dest.at[block], hop_sem.at[sems, RECV, index])

    dispatch(g, g_send)
    row_starts(g_send, g_rows, 0)

    def attend(i, _):
        s = (at.exp + 1 + i) % exps
        ok = lane_of((rows, rows)) < lengths[at.base + s]
        lane = lane_of((rows, block_cols))
        sums = jnp.zeros((rows, 128), full)
        for c in range(head_cols // block_cols):
            cols = slice(c * block_cols, (c + 1) * block_cols)
            q = qkv[s, :, cols]
            k = qkv[s, :, head_cols + c * block_cols : head_cols + (c + 1) * block_cols]
            v = qkv[s, :, 2 * head_cols + c * block_cols : 2 * head_cols + (c + 1) * block_cols]
            result = jnp.zeros((rows, block_cols), full)
            for t in range(block_cols // head_dim):
                h = c * (block_cols // head_dim) + t
                here = jnp.logical_and(lane >= t * head_dim, lane < (t + 1) * head_dim)
                scores = nt(jnp.where(here, q, jnp.zeros_like(q)), k) * scale + bias[h]
                scores = jnp.where(ok, scores, -1e30)
                top = jnp.max(scores, axis=1, keepdims=True)
                weights = jnp.exp(scores - top)
                total = jnp.sum(weights, axis=1, keepdims=True)
                weights = (weights * (1.0 / total)).astype(low)
                result = jnp.where(here, jnp.dot(weights, v, preferred_element_type=full), result)
                sums = jnp.where(lane_of((rows, 128)) == h, top + jnp.log(total), sums)
            mine[s, :, cols] = result.astype(low)
        lse[s] = sums

        @pl.when(i < exps - 1)
        def _():
            send(
                mine.at[s], ctx.at[at.exp], ctx_sem.at[SEND, s], ctx_sem.at[RECV, at.exp], at.device(at.rep, s)
            ).start()

        @pl.when(i == exps - 1)
        def _():
            pltpu.make_async_copy(mine.at[s], ctx.at[at.exp], ctx_sem.at[RECV, at.exp]).start()

        return 0

    lax.fori_loop(0, exps, attend, 0)

    rows_in(g_rows, 0)
    g_hops = hops(g_rows, 0, 1, 2)
    g_hops[0].start()
    g_hops[1].start()

    for k in range(1, exps):
        arrived(wout.at[exp_peer(k)], wo2_sem.at[RECV, exp_peer(k)])
    for e in range(exps):
        arrived(ctx.at[e], ctx_sem.at[RECV, e])

    out_cols = wout.shape[3]
    for r in range(reps):
        cols = slice(r * out_cols, (r + 1) * out_cols)
        total = tokens[:, cols].astype(full)
        for e in range(exps):
            total = total + jnp.dot(ctx[e], wout[e, r], preferred_element_type=full)
        h1_out[:, cols] = total
    h1 = h1_out[...]
    r2 = lax.rsqrt(jnp.mean(h1 * h1, axis=1, keepdims=True) + eps_norm)
    n2 = (h1 * r2 * gains[1:2, :]).astype(low)
    n2_out[...] = n2
    dispatch(n2, n_send)
    row_starts(n_send, n_rows, 1)

    logits = jnp.dot(n2.astype(full), router[...], precision=highest, preferred_element_type=full)
    lane = lane_of((rows, 128))
    logits = jnp.where(lane < exps, logits, -1e30)
    probs = jnp.exp(logits - jnp.max(logits, axis=1, keepdims=True))
    probs = probs / jnp.sum(probs, axis=1, keepdims=True)
    probs_out[...] = probs
    mine_hot = jnp.logical_or(lane == routes_col[:, 0:1], lane == routes_col[:, 1:2])
    picked = jnp.where(mine_hot, probs, 0.0)
    comb = picked / jnp.sum(picked, axis=1, keepdims=True)
    comb = jnp.where(valid, comb, 0.0)
    comb_out[...] = comb
    comb_t = comb.T
    for e in range(exps):
        line = nt(
            jnp.broadcast_to(comb_t[e : e + 1, :], (8, rows)), place[e].astype(full), precision=highest
        )
        comb_send[e] = jnp.zeros_like(comb_send[e])
        comb_send[e, :, 0:cap] = line
    row_starts(comb_send, comb_rows, 2)

    hop_in(g_rows, 0, 0, at.near(1))
    g_hops[2].start()

    rows_in(n_rows, 1)
    n_hops = hops(n_rows, 1, 2, 1)
    n_hops[0].start()
    n_hops[1].start()
    rows_in(comb_rows, 2)
    c_hops = hops(comb_rows, 2, 2, 1)
    c_hops[0].start()
    c_hops[1].start()

    stores = [
        (qkv, qkv_out),
        (lse, lse_out),
        (mine, mine_out),
        (n1, n1_out),
        (wqkv, wqkv_out),
        (wout, wout_out),
        (place, place_out),
    ]
    for i, (src, dst) in enumerate(stores):
        pltpu.make_async_copy(src, dst, store_sem.at[i]).start()

    hop_in(n_rows, 1, 0, at.near(2))
    n_hops[2].start()
    hop_in(comb_rows, 2, 0, at.near(2))
    c_hops[2].start()

    hop_in(g_rows, 0, 1, at.near(2))
    hop_in(g_rows, 0, 2, at.near(3))
    hop_in(n_rows, 1, 1, at.near(1))
    hop_in(n_rows, 1, 2, at.near(3))
    hop_in(comb_rows, 2, 1, at.near(1))
    hop_in(comb_rows, 2, 2, at.near(3))

    def weights_in(r, _):
        here = pl.ds(pl.multiple_of(r * slab, slab), slab)
        arrived(gate_w.at[here], weight_sem.at[RECV, r])
        arrived(up_w.at[here], weight2_sem.at[RECV, r])
        return 0

    lax.fori_loop(0, reps, weights_in, 0)
    for k in range(grps):
        arrived(down_w.at[k], weight_sem.at[RECV, reps + k])

    for k in range(1, exps):
        peer = exp_peer(k)
        arrived(tokens, tok_sem.at[SEND, peer])
        arrived(cotangent, cot_sem.at[SEND, peer])
        arrived(mine.at[peer], ctx_sem.at[SEND, peer])
    over_segments(lambda copy: copy.wait_send(), lambda k, src, dst: None)
    for k in range(1, reps):
        arrived(out_w, wo_sem.at[SEND, (at.rep + k) % reps])
    for copies in (
        wout_copies(),
        row_copies(g_send, g_rows, 0),
        row_copies(n_send, n_rows, 1),
        row_copies(comb_send, comb_rows, 2),
        g_hops,
        n_hops,
        c_hops,
        down_copies(),
    ):
        for copy in copies:
            copy.wait_send()

    def sent_weights(k, _):
        for copy in weight_copies(k):
            copy.wait_send()
        return 0

    lax.fori_loop(1, reps, sent_weights, 0)
    for i, (src, dst) in enumerate(stores):
        pltpu.make_async_copy(src, dst, store_sem.at[i]).wait()


def forward_call(
    grps, exps, cap, lengths, deal, rel_bias, routes_row, routes_col, tokens, cotangent, gains, router,
    qkv_t, out_w, gate_pieces, up_pieces, down_slab
):
    reps = grps * QUAD
    rows, width = tokens.shape
    head_cols = width // exps
    row_block = qkv_t.shape[1]
    seg = math.gcd(qkv_t.shape[0], head_cols)
    segs = qkv_t.shape[0] // seg
    slab, quarter = gate_pieces.shape[1:]
    units = down_slab.shape[0]
    out_cols = out_w.shape[1]
    heads = HEADS // exps
    cap_lanes = -(-cap // 128) * 128
    shape = jax.ShapeDtypeStruct
    vmem = pl.BlockSpec(memory_space=pltpu.VMEM)
    smem = pl.BlockSpec(memory_space=pltpu.SMEM)
    hbm = pl.BlockSpec(memory_space=pl.ANY)
    results = [
        (shape((width, quarter), low), hbm),
        (shape((width, quarter), low), hbm),
        (shape((grps, units, width), low), hbm),
        (shape((QUAD, exps, cap, width), low), hbm),
        (shape((QUAD, exps, cap, width), low), hbm),
        (shape((QUAD, exps, 8, cap_lanes), full), hbm),
        (shape((exps, rows, 3 * head_cols), low), hbm),
        (shape((exps, rows, 128), full), hbm),
        (shape((exps, rows, head_cols), low), hbm),
        (shape((exps, rows, width), low), hbm),
        (shape((exps, 3 * head_cols, row_block), low), hbm),
        (shape((exps, reps, row_block, out_cols), low), hbm),
        (shape((rows, width), full), vmem),
        (shape((rows, width), low), vmem),
        (shape((rows, width), low), vmem),
        (shape((rows, 128), full), vmem),
        (shape((rows, 128), full), vmem),
        (shape((exps, cap, rows), low), hbm),
    ]
    dma = pltpu.SemaphoreType.DMA
    return pl.pallas_call(
        functools.partial(forward_kernel, grps, exps, cap),
        out_shape=[r[0] for r in results],
        in_specs=[smem] * 3 + [vmem] * 8 + [hbm] * 3,
        out_specs=[r[1] for r in results],
        scratch_shapes=[
            pltpu.VMEM((exps, rows, width), low),
            pltpu.VMEM((exps, rows, width), low),
            pltpu.VMEM((exps, 3 * head_cols, row_block), low),
            pltpu.VMEM((exps, reps, row_block, out_cols), low),
            pltpu.VMEM((exps, rows, width), low),
            pltpu.VMEM((exps, rows, 3 * head_cols), low),
            pltpu.VMEM((exps, rows, 128), full),
            pltpu.VMEM((exps, rows, head_cols), low),
            pltpu.VMEM((exps, rows, head_cols), low),
            pltpu.VMEM((heads, rows, rows), full),
            pltpu.VMEM((exps, cap, rows), low),
            pltpu.VMEM((exps, cap, width), low),
            pltpu.VMEM((exps, cap, width), low),
            pltpu.VMEM((exps, 8, cap_lanes), full),
            dma((2, exps)),
            dma((2, exps)),
            dma((2, max(segs * reps, exps * 3 * head_cols // seg))),
            dma((2, reps)),
            dma((2, exps)),
            dma((2, reps + grps)),
            dma((2, reps)),
            dma((2, exps)),
            dma((3, 2, exps)),
            dma((3, 2, 3)),
            dma((7,)),
        ],
        compiler_params=pltpu.CompilerParams(
            collective_id=0, has_side_effects=True, vmem_limit_bytes=60 * 1024 * 1024
        ),
        name="forward",
    )(
        lengths, deal, rel_bias, routes_row, routes_col, tokens, cotangent, gains, router, qkv_t, out_w,
        gate_pieces, up_pieces, down_slab
    )


def per_device(
    tokens,
    cotangent,
    seq_lengths,
    deal,
    routes,
    attn_qkv,
    qkv_first,
    qkv_second,
    attn_out,
    out_first,
    out_second,
    rel_bias,
    bias_first,
    bias_second,
    router,
    router_first,
    router_second,
    norm_gains,
    gains_first,
    gains_second,
    expert_in,
    in_first,
    in_second,
    expert_out,
    down_first,
    down_second,
):
    rows, width = tokens.shape
    head_dim = width // HEADS
    score_scale = 1.0 / math.sqrt(head_dim)
    experts = router.shape[1]
    capacity = (10 * rows + 4 * experts - 1) // (4 * experts)
    exps = lax.axis_size("exp")
    grps = lax.axis_size("grp")
    reps = grps * QUAD
    heads = HEADS // exps
    head_cols = heads * head_dim
    place_index = lax.axis_index("exp")
    base = lax.axis_index(REP) * exps
    me = base + place_index

    units = expert_out.shape[1]
    slab = expert_in.shape[1]
    quarter = grps * units
    row_block = attn_qkv.shape[0]
    slots = experts * capacity

    my_routes = lax.dynamic_slice_in_dim(routes, me * rows, rows, 0)
    routes_row = jnp.zeros((8, rows), jnp.int32).at[:2].set(my_routes.T)
    routes_col = jnp.zeros((rows, 128), jnp.int32).at[:, :2].set(my_routes)
    gains = jnp.zeros((8, width), full).at[:2].set(norm_gains.T)
    router_wide = jnp.zeros((width, 128), full).at[:, :experts].set(router)
    shard_in = expert_in[0].astype(low).reshape(slab, 2, grps, QUAD, units)
    in_pieces = jnp.transpose(shard_in, (1, 3, 0, 2, 4)).reshape(2, QUAD, slab, quarter)
    (
        gate_mine, up_mine, down_mine, g_rows, n_rows, comb_rows, qkv, lse, context_mine, normed_group,
        wqkv, wout, hidden_one, normed_two, my_cotangent, router_probs, combine, place,
    ) = forward_call(
        grps, exps, capacity, seq_lengths, deal, rel_bias, routes_row, routes_col, tokens, cotangent, gains,
        router_wide, attn_qkv.astype(low).T, attn_out.astype(low), in_pieces[0], in_pieces[1],
        expert_out[0].astype(low),
    )
    down_mine = down_mine.reshape(quarter, width)
    expert_upstream = g_rows.reshape(-1, width)
    expert_rows = n_rows.reshape(-1, width)
    expert_combine = comb_rows[:, :, 0, :capacity].reshape(-1, 1)
    qkv_mine = jnp.transpose(wqkv, (0, 2, 1)).reshape(width, 3 * head_cols)
    full_out = jnp.transpose(wout, (0, 2, 1, 3)).reshape(width, width)
    normed_group = normed_group.reshape(exps * rows, width)
    qkv = qkv.reshape(exps, rows, 3, heads, head_dim)
    queries, key_rows, values = qkv[:, :, 0], qkv[:, :, 1], qkv[:, :, 2]
    log_total = jnp.transpose(lse[:, :, :heads], (0, 2, 1))[..., None]
    upstream = my_cotangent.astype(full)
    combine = combine[:, :experts]
    router_probs = router_probs[:, :experts]
    normed_float = normed_two.astype(full)
    places = jnp.arange(rows, dtype=jnp.int32)
    valid_rows = (places < seq_lengths[me]).astype(full)
    group_lengths = lax.dynamic_slice_in_dim(seq_lengths, base, exps, 0)
    key_ok = places[None, :] < group_lengths[:, None]
    gain_one = norm_gains[:, 0]
    gain_two = norm_gains[:, 1]
    chosen = (
        (my_routes[:, :, None] == jnp.arange(experts, dtype=jnp.int32)[None, None, :]).sum(axis=1).astype(full)
    )
    onehot = bucket_onehot(rows)
    bias_mine = lax.dynamic_slice_in_dim(rel_bias, place_index * heads, heads, 1)
    bias_table = jnp.einsum("ijb,bh->hij", onehot, bias_mine, precision=highest)

    def scores_of():
        raw = (
            jnp.einsum("sihd,sjhd->shij", queries, key_rows, preferred_element_type=full)
            * score_scale
            + bias_table[None]
        )
        return jnp.where(key_ok[:, None, None, :], raw, -1e30)

    x_float = tokens.astype(full)
    scale_one = lax.rsqrt(jnp.mean(x_float * x_float, axis=-1, keepdims=True) + eps_norm)
    scale_two = lax.rsqrt(jnp.mean(hidden_one * hidden_one, axis=-1, keepdims=True) + eps_norm)
    active_grad_bare = lax.dot_general(
        expert_upstream, down_mine, (((1,), (1,)), ((), ())), preferred_element_type=full
    )

    gate_part = dot(expert_rows, gate_mine)
    up_part = dot(expert_rows, up_mine)
    active_float, active_pull = jax.vjp(gated_unit, gate_part, up_part)
    active_scaled = (active_float * expert_combine).astype(low)
    combine_grad_part = jnp.sum(active_float * active_grad_bare, axis=-1).reshape(
        QUAD * experts, 1, capacity
    )
    gate_part_grad, up_part_grad = active_pull(active_grad_bare * expert_combine)
    gate_part_grad = gate_part_grad.astype(low)
    up_part_grad = up_part_grad.astype(low)
    rows_grad_part = (
        lax.dot_general(gate_part_grad, gate_mine, (((1,), (1,)), ((), ())), preferred_element_type=full)
        + lax.dot_general(up_part_grad, up_mine, (((1,), (1,)), ((), ())), preferred_element_type=full)
    ).astype(low)
    output_part = dot(active_scaled, down_mine).astype(low)

    combine_grad_back = swap(combine_grad_part, PLANE)
    rows_grad_back = swap(rows_grad_part.reshape(QUAD * experts, capacity, width), PLANE)
    output_back = swap(output_part.reshape(QUAD * experts, capacity, width), PLANE)

    def transposed_dot(a, b):
        return lax.dot_general(a, b, (((0,), (0,)), ((), ())), preferred_element_type=full)

    down_grad = transposed_dot(active_scaled, expert_upstream).astype(low)
    gate_grad = transposed_dot(expert_rows, gate_part_grad).astype(low)
    up_grad = transposed_dot(expert_rows, up_part_grad).astype(low)
    down_share = jnp.sum(
        swap(down_grad.reshape(grps, units, width), "grp").astype(full), axis=0
    )[None]

    def in_columns(grad):
        back = swap(grad.reshape(reps, slab, quarter), REP).astype(full)
        back = jnp.sum(back.reshape(grps, QUAD, slab, grps, units), axis=0)
        return jnp.transpose(back, (1, 2, 0, 3)).reshape(slab, grps * QUAD * units)

    in_share = jnp.concatenate([in_columns(gate_grad), in_columns(up_grad)], axis=1)[None]

    hot = jnp.broadcast_to(place[None], (QUAD,) + place.shape).reshape(-1, rows)

    def from_slots(parts):
        return lax.dot_general(
            hot, parts.reshape(-1, width), (((0,), (0,)), ((), ())), preferred_element_type=full
        )

    mixture = from_slots(output_back)
    block_loader = (valid_rows[:, None] * (hidden_one + mixture)).astype(low)
    seq_ids = jnp.arange(deal.shape[0], dtype=jnp.int32)
    dealt_seq = jnp.sum(jnp.where(deal == me, seq_ids, 0))
    block_out = lax.dynamic_index_in_dim(
        spread(block_loader, "exp"), dealt_seq - base, 0, keepdims=False
    )

    combine_grad_slots = jnp.sum(combine_grad_back.reshape(QUAD, experts, capacity), axis=0)
    combine_grad = jnp.einsum("ect,ec->te", place.astype(full), combine_grad_slots, precision=highest)
    gate_grad_value = combine_grad * valid_rows[:, None]
    gate_total = jnp.sum(router_probs * chosen, axis=-1, keepdims=True)
    gate_value = router_probs * chosen / gate_total
    probs_grad = chosen * (
        gate_grad_value - jnp.sum(gate_grad_value * gate_value, axis=-1, keepdims=True)
    ) / gate_total
    logit_grad = router_probs * (
        probs_grad - jnp.sum(probs_grad * router_probs, axis=-1, keepdims=True)
    )
    router_grad = jnp.dot(normed_float.T, logit_grad, precision=highest)
    normed_grad = jnp.dot(logit_grad, router.T, precision=highest) + from_slots(rows_grad_back)
    scaled_two = normed_grad * gain_two
    hidden_grad = (
        upstream
        + scale_two * scaled_two
        - hidden_one * scale_two**3 * jnp.mean(scaled_two * hidden_one, axis=-1, keepdims=True)
    )
    gain_two_grad = jnp.sum(normed_grad * hidden_one * scale_two, axis=0)
    branch_grad = hidden_grad.astype(low)
    context_grad = lax.dot_general(
        branch_grad, full_out, (((1,), (1,)), ((), ())), preferred_element_type=full
    ).astype(low)
    context_grad_pieces = jnp.transpose(context_grad.reshape(rows, exps, head_cols), (1, 0, 2))
    context_grad_mine = swap(context_grad_pieces, "exp").reshape(exps, rows, heads, head_dim)
    branch_group = spread(branch_grad, "exp").reshape(exps * rows, width)
    out_grad = transposed_dot(context_mine.reshape(exps * rows, head_cols), branch_group).astype(low)

    scores = scores_of()
    probs_again = jnp.exp(scores - log_total)
    weights_again = probs_again.astype(low)
    values_grad = jnp.einsum(
        "shij,sihd->sjhd", weights_again, context_grad_mine, preferred_element_type=full
    )
    probs_grad_att = jnp.einsum(
        "sihd,sjhd->shij", context_grad_mine, values, preferred_element_type=full
    )
    row_delta = jnp.sum(probs_grad_att * probs_again, axis=-1, keepdims=True)
    scores_grad = (probs_again * (probs_grad_att - row_delta)).astype(low)
    scores_grad_sum = jnp.sum(scores_grad.astype(full), axis=0)
    bias_grad_mine = jnp.einsum("hij,ijb->bh", scores_grad_sum, onehot, precision=highest)
    bias_grad = lax.dynamic_update_slice_in_dim(
        jnp.zeros((BUCKETS, HEADS), full), bias_grad_mine, place_index * heads, 1
    )
    queries_grad = (
        jnp.einsum("shij,sjhd->sihd", scores_grad, key_rows, preferred_element_type=full)
        * score_scale
    )
    keys_grad = (
        jnp.einsum("shij,sihd->sjhd", scores_grad, queries, preferred_element_type=full)
        * score_scale
    )
    qkv_grad = (
        jnp.stack([queries_grad, keys_grad, values_grad], axis=2)
        .astype(low)
        .reshape(exps * rows, 3 * head_cols)
    )
    normed_one_part = lax.dot_general(
        qkv_grad, qkv_mine, (((1,), (1,)), ((), ())), preferred_element_type=full
    ).astype(low)
    normed_one_grad = jnp.sum(
        swap(normed_one_part.reshape(exps, rows, width), "exp").astype(full), axis=0
    )
    scaled_one = normed_one_grad * gain_one
    token_grad = (
        hidden_grad
        + scale_one * scaled_one
        - x_float * scale_one**3 * jnp.mean(scaled_one * x_float, axis=-1, keepdims=True)
    )
    gain_one_grad = jnp.sum(normed_one_grad * x_float * scale_one, axis=0)

    qkv_weight_grad = transposed_dot(normed_group, qkv_grad).astype(low)
    qkv_grad_rows = swap(qkv_weight_grad.reshape(exps, row_block, 3 * head_cols), "exp")
    qkv_grad_rows = jnp.transpose(
        qkv_grad_rows.reshape(exps, row_block, 3, head_cols), (1, 2, 0, 3)
    ).reshape(row_block, reps, -1)
    qkv_share = jnp.sum(
        swap(jnp.transpose(qkv_grad_rows, (1, 0, 2)), REP).astype(full), axis=0
    )
    out_pieces = jnp.transpose(out_grad.reshape(row_block, reps, -1), (1, 0, 2))
    out_share = jnp.sum(swap(out_pieces, REP).astype(full), axis=0)

    small = jnp.concatenate(
        [
            router_grad.reshape(-1),
            jnp.stack([gain_one_grad, gain_two_grad], axis=1).reshape(-1),
            bias_grad.reshape(-1),
        ]
    ).reshape(-1, 128)
    small_total = jnp.sum(lax.all_gather(small, ALL, axis=0, tiled=False), axis=0).reshape(-1)
    router_total = small_total[: router.size].reshape(router.shape)
    gains_total = small_total[router.size : router.size + norm_gains.size].reshape(norm_gains.shape)
    bias_total = small_total[router.size + norm_gains.size :].reshape(rel_bias.shape)

    qkv_new = adamw_update(attn_qkv, qkv_first, qkv_second, qkv_share, 1.5 / math.sqrt(D), 0.1)
    out_new = adamw_update(attn_out, out_first, out_second, out_share, 6.0 / math.sqrt(D), 0.1)
    bias_new = adamw_update(rel_bias, bias_first, bias_second, bias_total, 0.3, 0.0)
    router_new = adamw_update(
        router, router_first, router_second, router_total, 1.0 / math.sqrt(D), 0.1
    )
    gains_new = adamw_update(norm_gains, gains_first, gains_second, gains_total, 0.5, 0.0)
    in_new = adamw_update(expert_in, in_first, in_second, in_share, 1.5 / math.sqrt(D), 0.1)
    down_new = adamw_update(
        expert_out, down_first, down_second, down_share, 1.5 / math.sqrt(FF), 0.1
    )
    return (
        (block_out, token_grad)
        + qkv_new
        + out_new
        + bias_new
        + router_new
        + gains_new
        + in_new
        + down_new
    )


def solution(mesh):
    reps, exps = mesh.devices.shape
    split = Mesh(mesh.devices.reshape(reps // QUAD, QUAD, exps), ALL)
    by_rows = P(ALL, None)
    attn = P("exp", REP)
    expert = P("exp", REP, None)
    return jax.shard_map(
        per_device,
        mesh=split,
        in_specs=(by_rows, by_rows) + (P(),) * 3 + (attn,) * 6 + (P(),) * 9 + (expert,) * 6,
        out_specs=(by_rows, by_rows) + (attn,) * 6 + (P(),) * 9 + (expert,) * 6,
        check_vma=False,
    )
```

```python
import functools
import math

import jax
import jax.numpy as jnp
from jax import lax
from jax.experimental import pallas as pl
from jax.experimental.pallas import tpu as pltpu
from jax.sharding import Mesh
from jax.sharding import PartitionSpec as P

D = 1024
HEADS = 16
FF = 2816
BUCKETS = 32
STEP = 10
QUAD = 4
REP = ("grp", "quad")
PLANE = ("quad", "exp")
ALL = ("grp", "quad", "exp")

highest = lax.Precision.HIGHEST
eps_norm = 1e-06
thresholds = (1, 2, 3, 4, 5, 6, 7, 8, 11, 16, 22, 32, 45, 64, 90)
beta_one = 0.9
beta_two = 0.999
eps_adam = 1e-08
low = jnp.bfloat16
full = jnp.float32
MESH = pl.DeviceIdType.MESH


def adamw_update(weight, moment, second, gradient, step_rate, decay_factor):
    new_moment = beta_one * moment + (1.0 - beta_one) * gradient
    new_second = beta_two * second + (1.0 - beta_two) * gradient * gradient
    corrected = new_moment / (1.0 - beta_one**STEP)
    scaled = new_second / (1.0 - beta_two**STEP)
    new_weight = weight - step_rate * (
        corrected / (jnp.sqrt(scaled) + eps_adam) + decay_factor * weight
    )
    return (new_moment, new_second, new_weight)


def gated_unit(gate_input, up_input):
    return jax.nn.gelu(gate_input, approximate=True) * up_input


def dot(a, b):
    return jnp.dot(a, b, preferred_element_type=full)


def nt(a, b, precision=None):
    return lax.dot_general(a, b, (((1,), (1,)), ((), ())), preferred_element_type=full, precision=precision)


def tn(a, b):
    return lax.dot_general(a, b, (((0,), (0,)), ((), ())), preferred_element_type=full)


class Where:
    def __init__(self, grps, exps):
        self.grps, self.exps = grps, exps
        self.reps = grps * QUAD
        self.grp = lax.axis_index("grp")
        self.quad = lax.axis_index("quad")
        self.exp = lax.axis_index("exp")
        self.rep = self.grp * QUAD + self.quad
        self.base = self.rep * exps
        self.me = self.base + self.exp

    def device(self, rep, exp):
        return (rep // QUAD, rep % QUAD, exp)

    def near(self, flip):
        q = self.quad
        if flip & 1:
            q = q + 1 - 2 * (q % 2)
        if flip & 2:
            q = q + 2 - 4 * (q // 2)
        return q


def send(src, dst, send_sem, recv_sem, device):
    return pltpu.make_async_remote_copy(
        src_ref=src, dst_ref=dst, send_sem=send_sem, recv_sem=recv_sem, device_id=device, device_id_type=MESH
    )


def arrived(ref, sem):
    pltpu.make_async_copy(ref, ref, sem).wait()


def greet_all(at):
    count = at.reps * at.exps
    barrier = pltpu.get_barrier_semaphore()

    def greet(k, _):
        other = (at.me + k) % count
        pl.semaphore_signal(
            barrier, inc=1, device_id=at.device(other // at.exps, other % at.exps), device_id_type=MESH
        )
        return 0

    lax.fori_loop(1, count, greet, 0)
    pl.semaphore_wait(barrier, count - 1)


def lane_of(shape):
    return lax.broadcasted_iota(jnp.int32, shape, 1)


def row_of(shape):
    return lax.broadcasted_iota(jnp.int32, shape, 0)


def bucket_of(offset):
    distance = jnp.abs(offset)
    bucket = jnp.where(offset > 0, 16, 0)
    for threshold in thresholds:
        bucket = bucket + jnp.where(distance >= threshold, 1, 0)
    return bucket


def forward_kernel(
    grps,
    exps,
    cap,
    lengths,
    deal,
    rel_bias,
    routes_row,
    routes_col,
    tokens,
    cotangent,
    gains,
    router,
    qkv_t,
    out_w,
    gate_pieces,
    up_pieces,
    down_slab,
    gate_w,
    up_w,
    down_w,
    g_rows,
    n_rows,
    comb_rows,
    qkv_out,
    lse_out,
    mine_out,
    n1_out,
    wqkv_out,
    wout_out,
    h1_out,
    n2_out,
    g_out,
    probs_out,
    comb_out,
    place_out,
    tok_all,
    cot_all,
    wqkv,
    wout,
    n1,
    qkv,
    lse,
    mine,
    ctx,
    bias,
    place,
    g_send,
    n_send,
    comb_send,
    tok_sem,
    cot_sem,
    wq_sem,
    wo_sem,
    wo2_sem,
    weight_sem,
    weight2_sem,
    ctx_sem,
    row_sem,
    hop_sem,
    store_sem,
):
    at = Where(grps, exps)
    reps = at.reps
    rows, width = tokens.shape
    heads = HEADS // exps
    head_dim = width // HEADS
    head_cols = heads * head_dim
    block_cols = min(128, head_cols)
    shard_cols, row_block = qkv_t.shape
    seg = math.gcd(shard_cols, head_cols)
    segs = shard_cols // seg
    slab = gate_pieces.shape[1]
    scale = 1.0 / math.sqrt(head_dim)
    SEND, RECV = 0, 1

    greet_all(at)

    def exp_peer(k):
        return (at.exp + k) % exps

    for k in range(1, exps):
        peer = exp_peer(k)
        send(
            tokens, tok_all.at[at.exp], tok_sem.at[SEND, peer], tok_sem.at[RECV, at.exp], at.device(at.rep, peer)
        ).start()
    tok_all[at.exp] = tokens[...]

    def segment(k):
        col = (at.rep * segs + k) * seg
        section = col // width
        within = col - section * width
        owner = within // head_cols
        return owner, section * head_cols + within - owner * head_cols

    def segment_copy(k, shift):
        owner, offset = segment(k)
        src = qkv_t.at[pl.ds(k * seg, seg)]
        dst = wqkv.at[at.exp, pl.ds(pl.multiple_of(offset, seg), seg)]
        target = at.device((at.rep + shift) % reps, owner)
        return owner, src, dst, send(
            src, dst, wq_sem.at[SEND, k * reps + shift], wq_sem.at[RECV, at.exp * 3 * (head_cols // seg) + offset // seg], target
        )

    def over_segments(act, act_local):
        def one(i, _):
            k, shift = i // reps, i % reps
            owner, src, dst, copy = segment_copy(k, shift)
            stays = jnp.logical_and(shift == 0, owner == at.exp)

            @pl.when(jnp.logical_not(stays))
            def _():
                act(copy)

            @pl.when(stays)
            def _():
                act_local(k, src, dst)

            return 0

        lax.fori_loop(0, segs * reps, one, 0)

    def local_segment(k, src, dst):
        _, offset = segment(k)
        pltpu.make_async_copy(src, dst, wq_sem.at[RECV, at.exp * 3 * (head_cols // seg) + offset // seg]).start()

    over_segments(lambda copy: copy.start(), local_segment)

    for k in range(1, reps):
        other = (at.rep + k) % reps
        send(
            out_w, wout.at[at.exp, at.rep], wo_sem.at[SEND, other], wo_sem.at[RECV, at.rep], at.device(other, at.exp)
        ).start()
    wout[at.exp, at.rep] = out_w[...]
    for k in range(1, exps):
        peer = exp_peer(k)
        send(
            cotangent, cot_all.at[at.exp], cot_sem.at[SEND, peer], cot_sem.at[RECV, at.exp], at.device(at.rep, peer)
        ).start()
    cot_all[at.exp] = cotangent[...]

    span = 2 * rows
    bucket = bucket_of(lane_of((8, span)) - rows)
    for h in range(heads):
        line = jnp.zeros((8, span), full)
        for b in range(BUCKETS):
            line = jnp.where(bucket == b, rel_bias[b, at.exp * heads + h], line)
        whole = jnp.broadcast_to(line[0:1], (rows, span))
        bias[h] = pltpu.roll(whole, 0, 1, stride=1, stride_axis=0)[:, rows:]

    first, second = routes_row[0:1, :], routes_row[1:2, :]
    expert_row = row_of((max(8, exps), rows))
    hot = jnp.logical_or(expert_row == first, expert_row == second)
    hot_low = jnp.where(hot, 1.0, 0.0).astype(low)
    earlier = jnp.where(row_of((rows, rows)) < lane_of((rows, rows)), 1.0, 0.0).astype(low)
    before = jnp.dot(hot_low, earlier, preferred_element_type=full)
    slot = row_of((cap, rows)).astype(full)
    for e in range(exps):
        inside = jnp.logical_and(slot == before[e : e + 1, :], hot_low[e : e + 1, :].astype(full) > 0.5)
        place[e] = jnp.where(inside, 1.0, 0.0).astype(low)

    def norm_group(s, _):
        @pl.when(s != at.exp)
        def _():
            arrived(tok_all.at[s], tok_sem.at[RECV, s])

        x = tok_all[s].astype(full)
        r = lax.rsqrt(jnp.mean(x * x, axis=1, keepdims=True) + eps_norm)
        n1[s] = (x * r * gains[0:1, :]).astype(low)
        return 0

    lax.fori_loop(0, exps, norm_group, 0)

    def wait_segment(i, _):
        e, j = i // (3 * head_cols // seg), i % (3 * head_cols // seg)
        arrived(wqkv.at[e, pl.ds(pl.multiple_of(j * seg, seg), seg)], wq_sem.at[RECV, i])
        return 0

    lax.fori_loop(0, exps * 3 * head_cols // seg, wait_segment, 0)

    def weight_copies(k):
        other = (at.rep + k) % reps
        device = at.device(other, at.exp)
        here = pl.ds(pl.multiple_of(at.rep * slab, slab), slab)
        return [
            send(
                gate_pieces.at[other % QUAD], gate_w.at[here], weight_sem.at[SEND, other], weight_sem.at[RECV, at.rep], device
            ),
            send(
                up_pieces.at[other % QUAD], up_w.at[here], weight2_sem.at[SEND, other], weight2_sem.at[RECV, at.rep], device
            ),
        ]

    def own_weights():
        here = pl.ds(pl.multiple_of(at.rep * slab, slab), slab)
        return [
            pltpu.make_async_copy(gate_pieces.at[at.quad], gate_w.at[here], weight_sem.at[RECV, at.rep]),
            pltpu.make_async_copy(up_pieces.at[at.quad], up_w.at[here], weight2_sem.at[RECV, at.rep]),
            pltpu.make_async_copy(down_slab, down_w.at[at.grp], weight_sem.at[RECV, reps + at.grp]),
        ]

    def down_copies():
        return [
            send(
                down_slab,
                down_w.at[at.grp],
                weight_sem.at[SEND, reps + (at.grp + k) % grps],
                weight_sem.at[RECV, reps + at.grp],
                ((at.grp + k) % grps, at.quad, at.exp),
            )
            for k in range(1, grps)
        ]

    for copy in down_copies():
        copy.start()

    def start_weights(k, _):
        for copy in weight_copies(k):
            copy.start()
        return 0

    lax.fori_loop(1, reps, start_weights, 0)
    for copy in own_weights():
        copy.start()

    def project(s, _):
        total = jnp.zeros((rows, 3 * head_cols), full)
        for e in range(exps):
            total = total + nt(n1[s, :, e * row_block : (e + 1) * row_block], wqkv[e])
        qkv[s] = total.astype(low)
        return 0

    lax.fori_loop(0, exps, project, 0)

    for k in range(1, reps):
        other = (at.rep + k) % reps
        arrived(wout.at[at.exp, other], wo_sem.at[RECV, other])

    def wout_copies():
        return [
            send(
                wout.at[at.exp],
                wout.at[at.exp],
                wo2_sem.at[SEND, exp_peer(k)],
                wo2_sem.at[RECV, at.exp],
                at.device(at.rep, exp_peer(k)),
            )
            for k in range(1, exps)
        ]

    for copy in wout_copies():
        copy.start()

    for k in range(1, exps):
        peer = exp_peer(k)
        arrived(cot_all.at[peer], cot_sem.at[RECV, peer])
    mine_place = deal[at.me] - at.base
    g = jnp.zeros((rows, width), full)
    for e in range(exps):
        g = jnp.where(mine_place == e, cot_all[e].astype(full), g)
    valid = row_of((rows, 1)) < lengths[at.me]
    g = jnp.where(valid, g, 0.0).astype(low)
    g_out[...] = g

    def dispatch(values, into):
        def one(e, _):
            into[e] = jnp.dot(place[e], values, preferred_element_type=full).astype(low)
            return 0

        lax.fori_loop(0, exps, one, 0)

    def row_copies(source, dest, sems):
        return [
            send(
                source.at[exp_peer(k)],
                dest.at[at.quad, at.exp],
                row_sem.at[sems, SEND, exp_peer(k)],
                row_sem.at[sems, RECV, at.exp],
                at.device(at.rep, exp_peer(k)),
            )
            for k in range(1, exps)
        ]

    def own_row_copy(source, dest, sems):
        return pltpu.make_async_copy(source.at[at.exp], dest.at[at.quad, at.exp], row_sem.at[sems, RECV, at.exp])

    def row_starts(source, dest, sems):
        for copy in row_copies(source, dest, sems):
            copy.start()
        own_row_copy(source, dest, sems).start()

    def rows_in(dest, sems):
        for e in range(exps):
            arrived(dest.at[at.quad, e], row_sem.at[sems, RECV, e])

    def hops(dest, sems, one, two):
        def hop(block, flip, index):
            return send(
                dest.at[block],
                dest.at[block],
                hop_sem.at[sems, SEND, index],
                hop_sem.at[sems, RECV, index],
                (at.grp, at.near(flip), at.exp),
            )

        return [hop(at.quad, one, 0), hop(at.quad, two, 1), hop(at.near(one), two, 2)]

    def hop_in(dest, sems, index, block):
        arrived(dest.at[block], hop_sem.at[sems, RECV, index])

    dispatch(g, g_send)
    row_starts(g_send, g_rows, 0)

    def attend(i, _):
        s = (at.exp + 1 + i) % exps
        ok = lane_of((rows, rows)) < lengths[at.base + s]
        lane = lane_of((rows, block_cols))
        sums = jnp.zeros((rows, 128), full)
        for c in range(head_cols // block_cols):
            cols = slice(c * block_cols, (c + 1) * block_cols)
            q = qkv[s, :, cols]
            k = qkv[s, :, head_cols + c * block_cols : head_cols + (c + 1) * block_cols]
            v = qkv[s, :, 2 * head_cols + c * block_cols : 2 * head_cols + (c + 1) * block_cols]
            result = jnp.zeros((rows, block_cols), full)
            for t in range(block_cols // head_dim):
                h = c * (block_cols // head_dim) + t
                here = jnp.logical_and(lane >= t * head_dim, lane < (t + 1) * head_dim)
                scores = nt(jnp.where(here, q, jnp.zeros_like(q)), k) * scale + bias[h]
                scores = jnp.where(ok, scores, -1e30)
                top = jnp.max(scores, axis=1, keepdims=True)
                weights = jnp.exp(scores - top)
                total = jnp.sum(weights, axis=1, keepdims=True)
                weights = (weights * (1.0 / total)).astype(low)
                result = jnp.where(here, jnp.dot(weights, v, preferred_element_type=full), result)
                sums = jnp.where(lane_of((rows, 128)) == h, top + jnp.log(total), sums)
            mine[s, :, cols] = result.astype(low)
        lse[s] = sums

        @pl.when(i < exps - 1)
        def _():
            send(
                mine.at[s], ctx.at[at.exp], ctx_sem.at[SEND, s], ctx_sem.at[RECV, at.exp], at.device(at.rep, s)
            ).start()

        @pl.when(i == exps - 1)
        def _():
            pltpu.make_async_copy(mine.at[s], ctx.at[at.exp], ctx_sem.at[RECV, at.exp]).start()

        return 0

    lax.fori_loop(0, exps, attend, 0)

    rows_in(g_rows, 0)
    g_hops = hops(g_rows, 0, 1, 2)
    g_hops[0].start()
    g_hops[1].start()

    for k in range(1, exps):
        arrived(wout.at[exp_peer(k)], wo2_sem.at[RECV, exp_peer(k)])
    for e in range(exps):
        arrived(ctx.at[e], ctx_sem.at[RECV, e])

    out_cols = wout.shape[3]
    for r in range(reps):
        cols = slice(r * out_cols, (r + 1) * out_cols)
        total = tokens[:, cols].astype(full)
        for e in range(exps):
            total = total + jnp.dot(ctx[e], wout[e, r], preferred_element_type=full)
        h1_out[:, cols] = total
    h1 = h1_out[...]
    r2 = lax.rsqrt(jnp.mean(h1 * h1, axis=1, keepdims=True) + eps_norm)
    n2 = (h1 * r2 * gains[1:2, :]).astype(low)
    n2_out[...] = n2
    dispatch(n2, n_send)
    row_starts(n_send, n_rows, 1)

    logits = jnp.dot(n2.astype(full), router[...], precision=highest, preferred_element_type=full)
    lane = lane_of((rows, 128))
    logits = jnp.where(lane < exps, logits, -1e30)
    probs = jnp.exp(logits - jnp.max(logits, axis=1, keepdims=True))
    probs = probs / jnp.sum(probs, axis=1, keepdims=True)
    probs_out[...] = probs
    mine_hot = jnp.logical_or(lane == routes_col[:, 0:1], lane == routes_col[:, 1:2])
    picked = jnp.where(mine_hot, probs, 0.0)
    comb = picked / jnp.sum(picked, axis=1, keepdims=True)
    comb = jnp.where(valid, comb, 0.0)
    comb_out[...] = comb
    comb_t = comb.T
    for e in range(exps):
        line = nt(
            jnp.broadcast_to(comb_t[e : e + 1, :], (8, rows)), place[e].astype(full), precision=highest
        )
        comb_send[e] = jnp.zeros_like(comb_send[e])
        comb_send[e, :, 0:cap] = line
    row_starts(comb_send, comb_rows, 2)

    hop_in(g_rows, 0, 0, at.near(1))
    g_hops[2].start()

    rows_in(n_rows, 1)
    n_hops = hops(n_rows, 1, 2, 1)
    n_hops[0].start()
    n_hops[1].start()
    rows_in(comb_rows, 2)
    c_hops = hops(comb_rows, 2, 2, 1)
    c_hops[0].start()
    c_hops[1].start()

    stores = [
        (qkv, qkv_out),
        (lse, lse_out),
        (mine, mine_out),
        (n1, n1_out),
        (wqkv, wqkv_out),
        (wout, wout_out),
        (place, place_out),
    ]
    for i, (src, dst) in enumerate(stores):
        pltpu.make_async_copy(src, dst, store_sem.at[i]).start()

    hop_in(n_rows, 1, 0, at.near(2))
    n_hops[2].start()
    hop_in(comb_rows, 2, 0, at.near(2))
    c_hops[2].start()

    hop_in(g_rows, 0, 1, at.near(2))
    hop_in(g_rows, 0, 2, at.near(3))
    hop_in(n_rows, 1, 1, at.near(1))
    hop_in(n_rows, 1, 2, at.near(3))
    hop_in(comb_rows, 2, 1, at.near(1))
    hop_in(comb_rows, 2, 2, at.near(3))

    def weights_in(r, _):
        here = pl.ds(pl.multiple_of(r * slab, slab), slab)
        arrived(gate_w.at[here], weight_sem.at[RECV, r])
        arrived(up_w.at[here], weight2_sem.at[RECV, r])
        return 0

    lax.fori_loop(0, reps, weights_in, 0)
    for k in range(grps):
        arrived(down_w.at[k], weight_sem.at[RECV, reps + k])

    for k in range(1, exps):
        peer = exp_peer(k)
        arrived(tokens, tok_sem.at[SEND, peer])
        arrived(cotangent, cot_sem.at[SEND, peer])
        arrived(mine.at[peer], ctx_sem.at[SEND, peer])
    over_segments(lambda copy: copy.wait_send(), lambda k, src, dst: None)
    for k in range(1, reps):
        arrived(out_w, wo_sem.at[SEND, (at.rep + k) % reps])
    for copies in (
        wout_copies(),
        row_copies(g_send, g_rows, 0),
        row_copies(n_send, n_rows, 1),
        row_copies(comb_send, comb_rows, 2),
        g_hops,
        n_hops,
        c_hops,
        down_copies(),
    ):
        for copy in copies:
            copy.wait_send()

    def sent_weights(k, _):
        for copy in weight_copies(k):
            copy.wait_send()
        return 0

    lax.fori_loop(1, reps, sent_weights, 0)
    for i, (src, dst) in enumerate(stores):
        pltpu.make_async_copy(src, dst, store_sem.at[i]).wait()


def forward_call(
    grps, exps, cap, lengths, deal, rel_bias, routes_row, routes_col, tokens, cotangent, gains, router,
    qkv_t, out_w, gate_pieces, up_pieces, down_slab
):
    reps = grps * QUAD
    rows, width = tokens.shape
    head_cols = width // exps
    row_block = qkv_t.shape[1]
    seg = math.gcd(qkv_t.shape[0], head_cols)
    segs = qkv_t.shape[0] // seg
    slab, quarter = gate_pieces.shape[1:]
    units = down_slab.shape[0]
    out_cols = out_w.shape[1]
    heads = HEADS // exps
    cap_lanes = -(-cap // 128) * 128
    shape = jax.ShapeDtypeStruct
    vmem = pl.BlockSpec(memory_space=pltpu.VMEM)
    smem = pl.BlockSpec(memory_space=pltpu.SMEM)
    hbm = pl.BlockSpec(memory_space=pl.ANY)
    results = [
        (shape((width, quarter), low), hbm),
        (shape((width, quarter), low), hbm),
        (shape((grps, units, width), low), hbm),
        (shape((QUAD, exps, cap, width), low), hbm),
        (shape((QUAD, exps, cap, width), low), hbm),
        (shape((QUAD, exps, 8, cap_lanes), full), hbm),
        (shape((exps, rows, 3 * head_cols), low), hbm),
        (shape((exps, rows, 128), full), hbm),
        (shape((exps, rows, head_cols), low), hbm),
        (shape((exps, rows, width), low), hbm),
        (shape((exps, 3 * head_cols, row_block), low), hbm),
        (shape((exps, reps, row_block, out_cols), low), hbm),
        (shape((rows, width), full), vmem),
        (shape((rows, width), low), vmem),
        (shape((rows, width), low), vmem),
        (shape((rows, 128), full), vmem),
        (shape((rows, 128), full), vmem),
        (shape((exps, cap, rows), low), hbm),
    ]
    dma = pltpu.SemaphoreType.DMA
    return pl.pallas_call(
        functools.partial(forward_kernel, grps, exps, cap),
        out_shape=[r[0] for r in results],
        in_specs=[smem] * 3 + [vmem] * 8 + [hbm] * 3,
        out_specs=[r[1] for r in results],
        scratch_shapes=[
            pltpu.VMEM((exps, rows, width), low),
            pltpu.VMEM((exps, rows, width), low),
            pltpu.VMEM((exps, 3 * head_cols, row_block), low),
            pltpu.VMEM((exps, reps, row_block, out_cols), low),
            pltpu.VMEM((exps, rows, width), low),
            pltpu.VMEM((exps, rows, 3 * head_cols), low),
            pltpu.VMEM((exps, rows, 128), full),
            pltpu.VMEM((exps, rows, head_cols), low),
            pltpu.VMEM((exps, rows, head_cols), low),
            pltpu.VMEM((heads, rows, rows), full),
            pltpu.VMEM((exps, cap, rows), low),
            pltpu.VMEM((exps, cap, width), low),
            pltpu.VMEM((exps, cap, width), low),
            pltpu.VMEM((exps, 8, cap_lanes), full),
            dma((2, exps)),
            dma((2, exps)),
            dma((2, max(segs * reps, exps * 3 * head_cols // seg))),
            dma((2, reps)),
            dma((2, exps)),
            dma((2, reps + grps)),
            dma((2, reps)),
            dma((2, exps)),
            dma((3, 2, exps)),
            dma((3, 2, 3)),
            dma((7,)),
        ],
        compiler_params=pltpu.CompilerParams(
            collective_id=0, has_side_effects=True, vmem_limit_bytes=60 * 1024 * 1024
        ),
        name="forward",
    )(
        lengths, deal, rel_bias, routes_row, routes_col, tokens, cotangent, gains, router, qkv_t, out_w,
        gate_pieces, up_pieces, down_slab
    )


def bits_of(count):
    return count.bit_length() - 1


def column_parts(width):
    tiles = width // 128
    cuts = [0, (tiles + 2) // 3, (2 * tiles + 2) // 3, tiles]
    return [(cuts[i] * 128, (cuts[i + 1] - cuts[i]) * 128) for i in range(3)]


class Halving:
    def __init__(self, at, source, kept, bufs, sems, load_sem):
        self.at, self.source, self.kept, self.bufs = at, source, kept, bufs
        self.sems, self.load_sem = sems, load_sem
        self.plane = at.quad * at.exps + at.exp
        self.places = bits_of(QUAD * at.exps)
        self.chip_bits = list(range(self.places - 1))
        self.parts = column_parts(source.shape[2])
        self.orders = [self.chip_bits[c:] + self.chip_bits[:c] for c in range(3)]

    def device(self, bit):
        mine = (self.plane // (1 << bit)) % 2
        other = self.plane + (1 - 2 * mine) * (1 << bit)
        return (self.at.grp, other // self.at.exps, other % self.at.exps)

    def first(self):
        core = self.plane % 2
        count = 1 << (self.places - 1)
        device = self.device(0)

        def copies(j):
            return send(
                self.source.at[2 * j + 1 - core], self.bufs[0].at[j], self.sems.at[0, 0, j], self.sems.at[0, 1, j], device
            )

        def load(j):
            return pltpu.make_async_copy(self.source.at[2 * j + core], self.kept.at[j], self.load_sem.at[j])

        return count, copies, load

    def start_first(self):
        count, copies, load = self.first()

        def one(j, _):
            copies(j).start()
            load(j).start()
            return 0

        lax.fori_loop(0, count, one, 0)

    def add_first(self):
        count, copies, load = self.first()

        def one(j, _):
            arrived(self.bufs[0].at[j], self.sems.at[0, 1, j])
            load(j).wait()
            self.bufs[0][j] = (self.bufs[0][j].astype(full) + self.kept[j].astype(full)).astype(low)
            return 0

        lax.fori_loop(0, count, one, 0)

    def hop(self, step, part):
        order = self.orders[part]
        bit = order[step]
        left = [b for b in self.chip_bits if b not in order[:step]]
        pos = left.index(bit)
        half = 1 << (len(left) - 1)
        mine = (self.plane // (1 << (bit + 1))) % 2
        device = self.device(bit + 1)
        begin, size = self.parts[part]
        cols = pl.ds(begin, size)
        base = self.base(step, part)

        def index(j, value):
            return (j >> pos) * (1 << (pos + 1)) + value * (1 << pos) + j % (1 << pos)

        pairs = []
        for j in range(half):
            copy = functools.partial(
                send,
                self.bufs[step].at[index(j, 1 - mine), :, cols],
                self.bufs[step + 1].at[j, :, cols],
                self.sems.at[1, 0, base + j],
                self.sems.at[1, 1, base + j],
                device,
            )
            pairs.append((copy, index(j, mine), j))
        return pairs, begin, size, base

    def base(self, step, part):
        n = len(self.chip_bits)
        return part * (1 << n) + sum(1 << (n - 1 - s) for s in range(step))

    def start(self, step, part=None):
        for p in range(3) if part is None else [part]:
            for copy, _, _ in self.hop(step, p)[0]:
                copy().start()

    def add(self, step, part):
        pairs, begin, size, base = self.hop(step, part)
        cols = pl.ds(begin, size)
        here, there = self.bufs[step], self.bufs[step + 1]
        for _, keep, j in pairs:
            arrived(there.at[j, :, cols], self.sems.at[1, 1, base + j])
            there[j, :, begin : begin + size] = (
                there[j, :, begin : begin + size].astype(full) + here[keep, :, begin : begin + size].astype(full)
            ).astype(low)

    def next(self, step):
        for p in range(3):
            self.add(step, p)
            if step + 1 < len(self.chip_bits):
                self.start(step + 1, p)

    def result(self):
        return self.bufs[len(self.chip_bits)]

    def finish(self):
        count, copies, _ = self.first()

        def one(j, _):
            copies(j).wait_send()
            return 0

        lax.fori_loop(0, count, one, 0)
        for step in range(len(self.chip_bits)):
            for p in range(3):
                for copy, _, _ in self.hop(step, p)[0]:
                    copy().wait_send()


def backward_kernel(
    grps,
    exps,
    lengths,
    deal,
    rel_bias,
    n_parts,
    y_parts,
    c_parts,
    gate_grad,
    up_grad,
    down_grad,
    n1_in,
    routes_col,
    tokens,
    gains,
    router,
    h1_in,
    n2_in,
    g_in,
    probs_in,
    qkv,
    lse,
    mine,
    wqkv,
    wout,
    token_grad,
    block_out,
    small_out,
    gate_parts,
    up_parts,
    down_parts,
    qkv_parts,
    out_parts,
    kept,
    n_bufs,
    y_bufs,
    c_in,
    dh1,
    dz_send,
    dz_all,
    do_send,
    do_in,
    bias,
    bias_sum,
    dqkv,
    dn1_send,
    dn1_in,
    n1,
    wq_send,
    og_send,
    blk_send,
    blk_in,
    small_send,
    small_exp,
    small_sum,
    small_rep,
    n_sem,
    y_sem,
    load_sem,
    c_sem,
    weight_sem,
    weight2_sem,
    dz_sem,
    do_sem,
    dn1_sem,
    wq_sem,
    og_sem,
    blk_sem,
    small_sem,
    small2_sem,
    n1_sem,
):
    at = Where(grps, exps)
    reps = at.reps
    rows, width = tokens.shape
    heads = HEADS // exps
    head_dim = width // HEADS
    head_cols = heads * head_dim
    block_cols = min(128, head_cols)
    row_block = wqkv.shape[2]
    out_cols = wout.shape[3]
    slab = gate_parts.shape[1]
    scale = 1.0 / math.sqrt(head_dim)
    SEND, RECV = 0, 1
    plane = at.quad * exps + at.exp
    members = QUAD * exps

    def exp_peer(k):
        return (at.exp + k) % exps

    greet_all(at)

    dn = Halving(at, n_parts, kept, n_bufs, n_sem, load_sem.at[0])
    ys = Halving(at, y_parts, kept, y_bufs, y_sem, load_sem.at[1])
    dn.start_first()
    n1_copy = pltpu.make_async_copy(n1_in, n1, n1_sem)
    n1_copy.start()

    def c_copy(k):
        other = (plane + k) % members
        return other, send(
            c_parts.at[other],
            c_in.at[plane],
            c_sem.at[SEND, other],
            c_sem.at[RECV, plane],
            (at.grp, other // exps, other % exps),
        )

    def start_c(k, _):
        c_copy(k)[1].start()
        return 0

    lax.fori_loop(1, members, start_c, 0)
    pltpu.make_async_copy(c_parts.at[plane], c_in.at[plane], c_sem.at[RECV, plane]).start()

    span = 2 * rows
    bucket = bucket_of(lane_of((8, span)) - rows)
    for h in range(heads):
        line = jnp.zeros((8, span), full)
        for b in range(BUCKETS):
            line = jnp.where(bucket == b, rel_bias[b, at.exp * heads + h], line)
        whole = jnp.broadcast_to(line[0:1], (rows, span))
        bias[h] = pltpu.roll(whole, 0, 1, stride=1, stride_axis=0)[:, rows:]

    dn.add_first()
    dn.start(0)
    ys.start_first()

    def wait_c(k, _):
        arrived(c_in.at[k], c_sem.at[RECV, k])
        return 0

    lax.fori_loop(0, members, wait_c, 0)
    lane = lane_of((rows, 128))
    comb_rows = []
    for e in range(exps):
        total = c_in[e]
        for q in range(1, QUAD):
            total = total + c_in[q * exps + e]
        comb_rows.append(total[0:1, :])
    comb_rows.append(jnp.zeros((128 - exps, rows), full))
    comb_grad = jnp.concatenate(comb_rows, axis=0).T
    valid = row_of((rows, 1)) < lengths[at.me]
    probs = probs_in[...]
    hot = jnp.logical_or(lane == routes_col[:, 0:1], lane == routes_col[:, 1:2])
    picked = jnp.where(hot, probs, 0.0)
    total = jnp.sum(picked, axis=1, keepdims=True)
    gate = picked / total
    gate_grad_rows = jnp.where(valid, comb_grad, 0.0)
    spread_grad = jnp.sum(gate_grad_rows * gate, axis=1, keepdims=True)
    probs_grad = jnp.where(hot, (gate_grad_rows - spread_grad) / total, 0.0)
    logit_grad = probs * (probs_grad - jnp.sum(probs_grad * probs, axis=1, keepdims=True))
    n2 = n2_in[...].astype(full)
    router_rows = lax.dot_general(
        logit_grad, n2, (((0,), (0,)), ((), ())), preferred_element_type=full, precision=highest
    )
    small_rows = small_send.shape[0]
    small_send[...] = jnp.zeros_like(small_send)
    small_send[0:exps, :] = router_rows[0:exps, :]
    router_back = nt(logit_grad, router[...], precision=highest)
    h1 = h1_in[...]
    r2 = lax.rsqrt(jnp.mean(h1 * h1, axis=1, keepdims=True) + eps_norm)

    dn.next(0)
    ys.add_first()
    dn.next(1)
    steps = len(dn.chip_bits)
    for step in range(2, steps):
        dn.next(step)

    def weight_copies(k):
        other = (at.rep + k) % reps
        device = at.device(other, at.exp)
        there = pl.ds(pl.multiple_of(other * slab, slab), slab)
        return [
            send(
                gate_grad.at[there], gate_parts.at[at.rep], weight_sem.at[SEND, other], weight_sem.at[RECV, at.rep], device
            ),
            send(
                up_grad.at[there], up_parts.at[at.rep], weight2_sem.at[SEND, other], weight2_sem.at[RECV, at.rep], device
            ),
        ]

    def down_copies():
        return [
            send(
                down_grad.at[(at.grp + k) % grps],
                down_parts.at[at.grp],
                weight_sem.at[SEND, reps + (at.grp + k) % grps],
                weight_sem.at[RECV, reps + at.grp],
                ((at.grp + k) % grps, at.quad, at.exp),
            )
            for k in range(1, grps)
        ]

    def start_weights(k, _):
        for copy in weight_copies(k):
            copy.start()
        return 0

    n2_grad = router_back + dn.result()[0].astype(full)
    scaled = n2_grad * gains[1:2, :]
    hidden_grad = (
        g_in[...].astype(full)
        + r2 * scaled
        - h1 * (r2 * r2 * r2) * jnp.mean(scaled * h1, axis=1, keepdims=True)
    )
    dh1[...] = hidden_grad
    small_send[exps + 1 : exps + 2, :] = jnp.sum(n2_grad * h1 * r2, axis=0, keepdims=True)
    branch = hidden_grad.astype(low)
    dz_send[...] = branch
    for e in range(exps):
        total = jnp.zeros((rows, row_block), full)
        for r in range(reps):
            total = total + nt(branch[:, r * out_cols : (r + 1) * out_cols], wout[e, r])
        do_send[e] = total.astype(low)

    def do_copies():
        return [
            send(
                do_send.at[exp_peer(k)],
                do_in.at[at.exp],
                do_sem.at[SEND, exp_peer(k)],
                do_sem.at[RECV, at.exp],
                at.device(at.rep, exp_peer(k)),
            )
            for k in range(1, exps)
        ]

    for copy in do_copies():
        copy.start()
    pltpu.make_async_copy(do_send.at[at.exp], do_in.at[at.exp], do_sem.at[RECV, at.exp]).start()

    def dz_copies():
        return [
            send(
                dz_send,
                dz_all.at[at.exp],
                dz_sem.at[SEND, exp_peer(k)],
                dz_sem.at[RECV, at.exp],
                at.device(at.rep, exp_peer(k)),
            )
            for k in range(1, exps)
        ]

    for copy in dz_copies():
        copy.start()
    dz_all[at.exp] = branch
    for copy in down_copies():
        copy.start()
    lax.fori_loop(1, reps, start_weights, 0)
    own_block = pl.ds(pl.multiple_of(at.rep * slab, slab), slab)
    own_copies = [
        pltpu.make_async_copy(gate_grad.at[own_block], gate_parts.at[at.rep], weight_sem.at[RECV, at.rep]),
        pltpu.make_async_copy(up_grad.at[own_block], up_parts.at[at.rep], weight2_sem.at[RECV, at.rep]),
        pltpu.make_async_copy(down_grad.at[at.grp], down_parts.at[at.grp], weight_sem.at[RECV, reps + at.grp]),
    ]
    for copy in own_copies:
        copy.start()
    ys.start(0)

    bias_sum[...] = jnp.zeros_like(bias_sum)

    def attend_back(i, _):
        s = (at.exp + 1 + i) % exps
        arrived(do_in.at[s], do_sem.at[RECV, s])
        ok = lane_of((rows, rows)) < lengths[at.base + s]
        block_lane = lane_of((rows, block_cols))
        for c in range(head_cols // block_cols):
            cols = slice(c * block_cols, (c + 1) * block_cols)
            k_cols = slice(head_cols + c * block_cols, head_cols + (c + 1) * block_cols)
            v_cols = slice(2 * head_cols + c * block_cols, 2 * head_cols + (c + 1) * block_cols)
            q = qkv[s, :, cols]
            k = qkv[s, :, k_cols]
            v = qkv[s, :, v_cols]
            do = do_in[s, :, cols]
            dq = jnp.zeros((rows, block_cols), full)
            dk = jnp.zeros((rows, block_cols), full)
            dv = jnp.zeros((rows, block_cols), full)
            for t in range(block_cols // head_dim):
                h = c * (block_cols // head_dim) + t
                here = jnp.logical_and(block_lane >= t * head_dim, block_lane < (t + 1) * head_dim)
                zero = jnp.zeros_like(q)
                q_h = jnp.where(here, q, zero)
                do_h = jnp.where(here, do, zero)
                scores = nt(q_h, k) * scale + bias[h]
                total = jnp.sum(jnp.where(lane == h, lse[s], 0.0), axis=1, keepdims=True)
                p = jnp.where(ok, jnp.exp(scores - total), 0.0)
                dp = nt(do_h, v)
                delta = jnp.sum(dp * p, axis=1, keepdims=True)
                ds = (p * (dp - delta)).astype(low)
                bias_sum[h] += ds.astype(full)
                dv = jnp.where(here, tn(p.astype(low), do), dv)
                dq = jnp.where(here, jnp.dot(ds, k, preferred_element_type=full), dq)
                dk = jnp.where(here, tn(ds, q), dk)
            dqkv[s, :, cols] = (dq * scale).astype(low)
            dqkv[s, :, k_cols] = (dk * scale).astype(low)
            dqkv[s, :, v_cols] = dv.astype(low)
        for e in range(exps):
            dn1_send[s, :, e * row_block : (e + 1) * row_block] = jnp.dot(
                dqkv[s], wqkv[e], preferred_element_type=full
            ).astype(low)

        @pl.when(i < exps - 1)
        def _():
            send(
                dn1_send.at[s], dn1_in.at[at.exp], dn1_sem.at[SEND, s], dn1_sem.at[RECV, at.exp], at.device(at.rep, s)
            ).start()

        @pl.when(i == exps - 1)
        def _():
            pltpu.make_async_copy(dn1_send.at[s], dn1_in.at[at.exp], dn1_sem.at[RECV, at.exp]).start()

        return 0

    lax.fori_loop(0, exps, attend_back, 0)

    n1_copy.wait()
    seg = wq_send.shape[2]
    segs = qkv_parts.shape[1]
    parts = wq_send.shape[1]
    for e in range(exps):
        total = jnp.zeros((3 * head_cols, row_block), full)
        for s in range(exps):
            total = total + tn(dqkv[s], n1[s, :, e * row_block : (e + 1) * row_block])
        for j in range(parts):
            wq_send[e, j] = total[j * seg : (j + 1) * seg].astype(low)

    def owner(j):
        section, within = j // (head_cols // seg), j % (head_cols // seg)
        col = section * width + at.exp * head_cols + within * seg
        block = col // seg
        return block // segs, block % segs

    def wq_copy(i):
        e, j = i // parts, i % parts
        rep, k = owner(j)
        dst = qkv_parts.at[at.rep, k]
        recv = wq_sem.at[RECV, at.rep * segs + k]
        stays = jnp.logical_and(rep == at.rep, e == at.exp)
        return (
            stays,
            functools.partial(send, wq_send.at[e, j], dst, wq_sem.at[SEND, i], recv, at.device(rep, e)),
            functools.partial(pltpu.make_async_copy, wq_send.at[e, j], dst, recv),
        )

    def start_wq(i, _):
        stays, away, local = wq_copy(i)

        @pl.when(stays)
        def _():
            local().start()

        @pl.when(jnp.logical_not(stays))
        def _():
            away().start()

        return 0

    lax.fori_loop(0, exps * parts, start_wq, 0)
    for k in range(1, exps):
        arrived(dz_all.at[exp_peer(k)], dz_sem.at[RECV, exp_peer(k)])
    for r in range(reps):
        total = jnp.zeros((head_cols, out_cols), full)
        for s in range(exps):
            total = total + tn(mine[s], dz_all[s, :, r * out_cols : (r + 1) * out_cols])
        og_send[r] = total.astype(low)

    def og_copies():
        return [
            send(
                og_send.at[(at.rep + k) % reps],
                out_parts.at[at.rep],
                og_sem.at[SEND, (at.rep + k) % reps],
                og_sem.at[RECV, at.rep],
                at.device((at.rep + k) % reps, at.exp),
            )
            for k in range(1, reps)
        ]

    for copy in og_copies():
        copy.start()
    pltpu.make_async_copy(og_send.at[at.rep], out_parts.at[at.rep], og_sem.at[RECV, at.rep]).start()

    line_lane = lane_of((8, 128))
    line_row = row_of((8, 128))
    bias_line = jnp.zeros((8, 128), full)
    flip = jnp.where(row_of((rows, rows)) + lane_of((rows, rows)) == rows - 1, 1.0, 0.0)
    turned_bucket = bucket_of(rows - 1 - lane_of((8, span)))
    for h in range(heads):
        flipped = jnp.dot(bias_sum[h], flip, precision=highest, preferred_element_type=full)
        square = jnp.concatenate([flipped, jnp.zeros((rows, rows), full)], axis=1)
        turned = pltpu.roll(square, 0, 1, stride=1, stride_axis=0)
        sums = jnp.broadcast_to(jnp.sum(turned, axis=0, keepdims=True), (8, span))
        for b in range(BUCKETS):
            value = jnp.sum(jnp.where(turned_bucket == b, sums, 0.0), axis=1, keepdims=True)
            bias_line = jnp.where(jnp.logical_and(line_row == h, line_lane == b), value, bias_line)
    for h in range(heads):
        small_send[exps + 2 : exps + 3, h * 128 : (h + 1) * 128] = bias_line[h : h + 1, :]

    ys.next(0)

    for e in range(exps):
        arrived(dn1_in.at[e], dn1_sem.at[RECV, e])
    n1_grad = dn1_in[0].astype(full)
    for e in range(1, exps):
        n1_grad = n1_grad + dn1_in[e].astype(full)
    x = tokens[...].astype(full)
    r1 = lax.rsqrt(jnp.mean(x * x, axis=1, keepdims=True) + eps_norm)
    scaled = n1_grad * gains[0:1, :]
    token_grad[...] = (
        dh1[...] + r1 * scaled - x * (r1 * r1 * r1) * jnp.mean(scaled * x, axis=1, keepdims=True)
    )
    small_send[exps : exps + 1, :] = jnp.sum(n1_grad * x * r1, axis=0, keepdims=True)

    def small_copies():
        return [
            send(
                small_send,
                small_exp.at[at.exp],
                small_sem.at[SEND, exp_peer(k)],
                small_sem.at[RECV, at.exp],
                at.device(at.rep, exp_peer(k)),
            )
            for k in range(1, exps)
        ]

    for copy in small_copies():
        copy.start()
    small_exp[at.exp] = small_send[...]
    for step in range(1, steps):
        ys.next(step)
    block = jnp.where(valid, h1_in[...] + ys.result()[0].astype(full), 0.0).astype(low)
    blk_send[...] = block

    def blk_copies():
        return [
            send(
                blk_send,
                blk_in.at[at.exp],
                blk_sem.at[SEND, exp_peer(k)],
                blk_sem.at[RECV, at.exp],
                at.device(at.rep, exp_peer(k)),
            )
            for k in range(1, exps)
        ]

    for copy in blk_copies():
        copy.start()
    blk_in[at.exp] = block
    for k in range(1, exps):
        arrived(small_exp.at[exp_peer(k)], small_sem.at[RECV, exp_peer(k)])
    total = small_exp[0]
    for e in range(1, exps):
        total = total + small_exp[e]
    small_sum[0] = total
    for e in range(exps):
        small_sum[0, exps + 3 + e : exps + 4 + e, :] = small_exp[e, exps + 2 : exps + 3, :]

    def small2_copies():
        return [
            send(
                small_sum.at[0],
                small_rep.at[at.rep],
                small2_sem.at[SEND, (at.rep + k) % reps],
                small2_sem.at[RECV, at.rep],
                at.device((at.rep + k) % reps, at.exp),
            )
            for k in range(1, reps)
        ]

    for copy in small2_copies():
        copy.start()
    small_rep[at.rep] = small_sum[0]
    for k in range(1, exps):
        arrived(blk_in.at[exp_peer(k)], blk_sem.at[RECV, exp_peer(k)])
    chosen = jnp.zeros((rows, width), full)
    for e in range(exps):
        chosen = jnp.where(deal[at.base + e] == at.me, blk_in[e].astype(full), chosen)
    block_out[...] = chosen.astype(low)
    for k in range(1, reps):
        arrived(small_rep.at[(at.rep + k) % reps], small2_sem.at[RECV, (at.rep + k) % reps])
    total = small_rep[0]
    for r in range(1, reps):
        total = total + small_rep[r]
    small_out[...] = total

    def weights_in(r, _):
        arrived(gate_parts.at[r], weight_sem.at[RECV, r])
        arrived(up_parts.at[r], weight2_sem.at[RECV, r])
        arrived(out_parts.at[r], og_sem.at[RECV, r])
        return 0

    lax.fori_loop(0, reps, weights_in, 0)
    for k in range(grps):
        arrived(down_parts.at[k], weight_sem.at[RECV, reps + k])

    def wq_in(i, _):
        arrived(qkv_parts.at[i // segs, i % segs], wq_sem.at[RECV, i])
        return 0

    lax.fori_loop(0, reps * segs, wq_in, 0)

    def sent_c(k, _):
        c_copy(k)[1].wait_send()
        return 0

    lax.fori_loop(1, members, sent_c, 0)
    dn.finish()
    ys.finish()

    def sent_weights(k, _):
        for copy in weight_copies(k):
            copy.wait_send()
        return 0

    lax.fori_loop(1, reps, sent_weights, 0)

    def sent_wq(i, _):
        stays, away, _ = wq_copy(i)

        @pl.when(jnp.logical_not(stays))
        def _():
            away().wait_send()

        return 0

    lax.fori_loop(0, exps * parts, sent_wq, 0)
    for copies in (
        down_copies(),
        do_copies(),
        dz_copies(),
        og_copies(),
        small_copies(),
        blk_copies(),
        small2_copies(),
    ):
        for copy in copies:
            copy.wait_send()
    for k in range(1, exps):
        arrived(dn1_send.at[exp_peer(k)], dn1_sem.at[SEND, exp_peer(k)])


def backward_call(
    grps, exps, lengths, deal, rel_bias, n_parts, y_parts, c_parts, gate_grad, up_grad, down_grad, n1, routes_col,
    tokens, gains, router, h1, n2, g, probs, qkv, lse, mine, wqkv, wout
):
    reps = grps * QUAD
    rows, width = tokens.shape
    heads = HEADS // exps
    head_cols = width // exps
    row_block = wqkv.shape[2]
    out_cols = wout.shape[3]
    shard_cols = 3 * width // reps
    seg = math.gcd(shard_cols, head_cols)
    segs = shard_cols // seg
    parts = 3 * head_cols // seg
    quarter = gate_grad.shape[1]
    slab = width // reps
    units = down_grad.shape[1]
    members = QUAD * exps
    chip_bits = bits_of(members) - 1
    small_rows = -(-(2 * exps + 3) // 8) * 8
    shape = jax.ShapeDtypeStruct
    vmem = pl.BlockSpec(memory_space=pltpu.VMEM)
    smem = pl.BlockSpec(memory_space=pltpu.SMEM)
    hbm = pl.BlockSpec(memory_space=pl.ANY)
    results = [
        (shape((rows, width), full), vmem),
        (shape((rows, width), low), vmem),
        (shape((small_rows, width), full), vmem),
        (shape((reps, slab, quarter), low), hbm),
        (shape((reps, slab, quarter), low), hbm),
        (shape((grps, units, width), low), hbm),
        (shape((reps, segs, seg, row_block), low), hbm),
        (shape((reps, row_block, out_cols), low), hbm),
    ]
    dma = pltpu.SemaphoreType.DMA
    bufs = [pltpu.VMEM((1 << (chip_bits - s), rows, width), low) for s in range(chip_bits + 1)]
    return pl.pallas_call(
        functools.partial(backward_kernel, grps, exps),
        out_shape=[r[0] for r in results],
        in_specs=[smem] * 3 + [hbm] * 7 + [vmem] * 13,
        out_specs=[r[1] for r in results],
        scratch_shapes=[
            pltpu.VMEM((members // 2, rows, width), low),
            list(bufs),
            list(bufs),
            pltpu.VMEM((members, 8, rows), full),
            pltpu.VMEM((rows, width), full),
            pltpu.VMEM((rows, width), low),
            pltpu.VMEM((exps, rows, width), low),
            pltpu.VMEM((exps, rows, head_cols), low),
            pltpu.VMEM((exps, rows, head_cols), low),
            pltpu.VMEM((heads, rows, rows), full),
            pltpu.VMEM((heads, rows, rows), full),
            pltpu.VMEM((exps, rows, 3 * head_cols), low),
            pltpu.VMEM((exps, rows, width), low),
            pltpu.VMEM((exps, rows, width), low),
            pltpu.VMEM((exps, rows, width), low),
            pltpu.VMEM((exps, parts, seg, row_block), low),
            pltpu.VMEM((reps, row_block, out_cols), low),
            pltpu.VMEM((rows, width), low),
            pltpu.VMEM((exps, rows, width), low),
            pltpu.VMEM((small_rows, width), full),
            pltpu.VMEM((exps, small_rows, width), full),
            pltpu.VMEM((1, small_rows, width), full),
            pltpu.VMEM((reps, small_rows, width), full),
            dma((2, 2, 3 << chip_bits)),
            dma((2, 2, 3 << chip_bits)),
            dma((2, members // 2)),
            dma((2, members)),
            dma((2, reps + grps)),
            dma((2, reps)),
            dma((2, exps)),
            dma((2, exps)),
            dma((2, exps)),
            dma((2, max(exps * parts, reps * segs))),
            dma((2, reps)),
            dma((2, exps)),
            dma((2, exps)),
            dma((2, reps)),
            dma,
        ],
        compiler_params=pltpu.CompilerParams(
            collective_id=1, has_side_effects=True, vmem_limit_bytes=60 * 1024 * 1024
        ),
        name="backward",
    )(
        lengths, deal, rel_bias, n_parts, y_parts, c_parts, gate_grad, up_grad, down_grad, n1, routes_col, tokens,
        gains, router, h1, n2, g, probs, qkv, lse, mine, wqkv, wout
    )


def per_device(
    tokens,
    cotangent,
    seq_lengths,
    deal,
    routes,
    attn_qkv,
    qkv_first,
    qkv_second,
    attn_out,
    out_first,
    out_second,
    rel_bias,
    bias_first,
    bias_second,
    router,
    router_first,
    router_second,
    norm_gains,
    gains_first,
    gains_second,
    expert_in,
    in_first,
    in_second,
    expert_out,
    down_first,
    down_second,
):
    rows, width = tokens.shape
    head_dim = width // HEADS
    score_scale = 1.0 / math.sqrt(head_dim)
    experts = router.shape[1]
    capacity = (10 * rows + 4 * experts - 1) // (4 * experts)
    exps = lax.axis_size("exp")
    grps = lax.axis_size("grp")
    reps = grps * QUAD
    heads = HEADS // exps
    head_cols = heads * head_dim
    place_index = lax.axis_index("exp")
    base = lax.axis_index(REP) * exps
    me = base + place_index

    units = expert_out.shape[1]
    slab = expert_in.shape[1]
    quarter = grps * units
    row_block = attn_qkv.shape[0]
    slots = experts * capacity

    my_routes = lax.dynamic_slice_in_dim(routes, me * rows, rows, 0)
    routes_row = jnp.zeros((8, rows), jnp.int32).at[:2].set(my_routes.T)
    routes_col = jnp.zeros((rows, 128), jnp.int32).at[:, :2].set(my_routes)
    gains = jnp.zeros((8, width), full).at[:2].set(norm_gains.T)
    router_wide = jnp.zeros((width, 128), full).at[:, :experts].set(router)
    shard_in = expert_in[0].astype(low).reshape(slab, 2, grps, QUAD, units)
    in_pieces = jnp.transpose(shard_in, (1, 3, 0, 2, 4)).reshape(2, QUAD, slab, quarter)
    (
        gate_mine, up_mine, down_mine, g_rows, n_rows, comb_rows, qkv, lse, context_mine, normed_group,
        wqkv, wout, hidden_one, normed_two, my_cotangent, router_probs, combine, place,
    ) = forward_call(
        grps, exps, capacity, seq_lengths, deal, rel_bias, routes_row, routes_col, tokens, cotangent, gains,
        router_wide, attn_qkv.astype(low).T, attn_out.astype(low), in_pieces[0], in_pieces[1],
        expert_out[0].astype(low),
    )
    down_mine = down_mine.reshape(quarter, width)
    expert_upstream = g_rows.reshape(-1, width)
    expert_rows = n_rows.reshape(-1, width)
    expert_combine = comb_rows[:, :, 0, :capacity].reshape(-1, 1)

    members = QUAD * exps
    group_routes = lax.dynamic_slice_in_dim(
        routes, (base - lax.axis_index("quad") * exps) * rows, members * rows, 0
    ).reshape(members, rows, 2)
    group_hot = jnp.any(group_routes == place_index, axis=-1)
    group_slot = jnp.cumsum(group_hot.astype(jnp.int32), axis=1) - 1
    slot_ids = jnp.arange(capacity, dtype=jnp.int32)
    group_place = jnp.logical_and(
        group_hot[:, None, :], group_slot[:, None, :] == slot_ids[None, :, None]
    )
    group_low = group_place.astype(low)

    def by_rows(parts):
        return jnp.einsum(
            "sct,scd->std", group_low, parts.reshape(members, capacity, width), preferred_element_type=full
        ).astype(low)

    active_grad_bare = lax.dot_general(
        expert_upstream, down_mine, (((1,), (1,)), ((), ())), preferred_element_type=full
    )
    gate_part = dot(expert_rows, gate_mine)
    up_part = dot(expert_rows, up_mine)
    active_float, active_pull = jax.vjp(gated_unit, gate_part, up_part)
    active_scaled = (active_float * expert_combine).astype(low)
    combine_grad_part = jnp.sum(active_float * active_grad_bare, axis=-1).reshape(members, capacity, 1)
    gate_part_grad, up_part_grad = active_pull(active_grad_bare * expert_combine)
    gate_part_grad = gate_part_grad.astype(low)
    up_part_grad = up_part_grad.astype(low)
    rows_grad_part = (
        lax.dot_general(gate_part_grad, gate_mine, (((1,), (1,)), ((), ())), preferred_element_type=full)
        + lax.dot_general(up_part_grad, up_mine, (((1,), (1,)), ((), ())), preferred_element_type=full)
    ).astype(low)
    output_part = dot(active_scaled, down_mine).astype(low)
    combine_parts = jnp.sum(jnp.where(group_place, combine_grad_part, 0.0), axis=1)
    combine_parts = jnp.broadcast_to(combine_parts[:, None, :], (members, 8, rows))

    def transposed_dot(a, b):
        return lax.dot_general(a, b, (((0,), (0,)), ((), ())), preferred_element_type=full)

    down_grad = transposed_dot(active_scaled, expert_upstream).astype(low).reshape(grps, units, width)
    gate_grad = transposed_dot(expert_rows, gate_part_grad).astype(low)
    up_grad = transposed_dot(expert_rows, up_part_grad).astype(low)
    (
        token_grad, block_out, small, gate_parts, up_parts, down_parts, qkv_parts, out_parts,
    ) = backward_call(
        grps, exps, seq_lengths, deal, rel_bias, by_rows(rows_grad_part), by_rows(output_part), combine_parts,
        gate_grad, up_grad, down_grad, normed_group, routes_col, tokens, gains, router_wide, hidden_one,
        normed_two, my_cotangent, router_probs, qkv, lse, context_mine, wqkv, wout,
    )
    down_share = jnp.sum(down_parts.astype(full), axis=0)[None]

    def in_columns(parts):
        total = jnp.sum(parts.astype(full).reshape(grps, QUAD, slab, grps, units), axis=0)
        return jnp.transpose(total, (1, 2, 0, 3)).reshape(slab, grps * QUAD * units)

    in_share = jnp.concatenate([in_columns(gate_parts), in_columns(up_parts)], axis=1)[None]
    qkv_share = jnp.sum(qkv_parts.astype(full), axis=0).reshape(-1, row_block).T
    out_share = jnp.sum(out_parts.astype(full), axis=0)
    router_total = small[:experts].T
    gains_total = small[exps : exps + 2].T
    bias_total = jnp.transpose(
        small[exps + 3 : 2 * exps + 3, : heads * 128].reshape(exps, heads, 128)[:, :, :BUCKETS], (2, 0, 1)
    ).reshape(BUCKETS, HEADS)

    qkv_new = adamw_update(attn_qkv, qkv_first, qkv_second, qkv_share, 1.5 / math.sqrt(D), 0.1)
    out_new = adamw_update(attn_out, out_first, out_second, out_share, 6.0 / math.sqrt(D), 0.1)
    bias_new = adamw_update(rel_bias, bias_first, bias_second, bias_total, 0.3, 0.0)
    router_new = adamw_update(
        router, router_first, router_second, router_total, 1.0 / math.sqrt(D), 0.1
    )
    gains_new = adamw_update(norm_gains, gains_first, gains_second, gains_total, 0.5, 0.0)
    in_new = adamw_update(expert_in, in_first, in_second, in_share, 1.5 / math.sqrt(D), 0.1)
    down_new = adamw_update(
        expert_out, down_first, down_second, down_share, 1.5 / math.sqrt(FF), 0.1
    )
    return (
        (block_out, token_grad)
        + qkv_new
        + out_new
        + bias_new
        + router_new
        + gains_new
        + in_new
        + down_new
    )


def bucket_onehot(length):
    places = jnp.arange(length, dtype=jnp.int32)
    offset = places[None, :] - places[:, None]
    distance = jnp.abs(offset)
    bucket = 16 * (offset > 0).astype(jnp.int32)
    for threshold in thresholds:
        bucket = bucket + (distance >= threshold).astype(jnp.int32)
    return (bucket[:, :, None] == jnp.arange(BUCKETS, dtype=jnp.int32)[None, None, :]).astype(full)


def swap(pieces, axes):
    return lax.all_to_all(pieces, axes, split_axis=0, concat_axis=0, tiled=True)


def spread(block, axes):
    members = lax.axis_size(axes)
    return swap(jnp.broadcast_to(block[None], (members,) + block.shape), axes)


def plain_device(
    tokens,
    cotangent,
    seq_lengths,
    deal,
    routes,
    attn_qkv,
    qkv_first,
    qkv_second,
    attn_out,
    out_first,
    out_second,
    rel_bias,
    bias_first,
    bias_second,
    router,
    router_first,
    router_second,
    norm_gains,
    gains_first,
    gains_second,
    expert_in,
    in_first,
    in_second,
    expert_out,
    down_first,
    down_second,
):
    rows, width = tokens.shape
    head_dim = width // HEADS
    score_scale = 1.0 / math.sqrt(head_dim)
    experts = router.shape[1]
    capacity = (10 * rows + 4 * experts - 1) // (4 * experts)
    exps = lax.axis_size("exp")
    grps = lax.axis_size("grp")
    reps = grps * QUAD
    heads = HEADS // exps
    head_cols = heads * head_dim
    place = lax.axis_index("exp")
    base = lax.axis_index(REP) * exps
    me = base + place
    slab = expert_in.shape[1]
    units = expert_out.shape[1]
    quarter = grps * units

    row_block = attn_qkv.shape[0]
    qkv_rows = lax.all_gather(attn_qkv.astype(low), REP, axis=1, tiled=True)
    out_rows = lax.all_gather(attn_out.astype(low), REP, axis=1, tiled=True)
    qkv_pieces = jnp.transpose(
        qkv_rows.reshape(row_block, 3, exps, head_cols), (2, 0, 1, 3)
    ).reshape(exps, row_block, 3 * head_cols)
    qkv_mine = swap(qkv_pieces, "exp").reshape(width, 3 * head_cols)
    full_out = spread(out_rows, "exp").reshape(width, width)

    group_tokens = spread(tokens, "exp")
    group_cotangent = spread(cotangent, "exp")
    my_cotangent = lax.dynamic_index_in_dim(group_cotangent, deal[me] - base, 0, keepdims=False)

    my_routes = lax.dynamic_slice_in_dim(routes, me * rows, rows, 0)
    places = jnp.arange(rows, dtype=jnp.int32)
    valid_rows = (places < seq_lengths[me]).astype(full)
    group_lengths = lax.dynamic_slice_in_dim(seq_lengths, base, exps, 0)
    key_ok = places[None, :] < group_lengths[:, None]
    gain_one = norm_gains[:, 0]
    gain_two = norm_gains[:, 1]

    chosen = (my_routes[:, :, None] == jnp.arange(experts, dtype=jnp.int32)[None, None, :]).astype(full)
    flat_routes = my_routes.reshape(-1)
    route_hot = (flat_routes[:, None] == jnp.arange(experts, dtype=jnp.int32)[None, :]).astype(jnp.int32)
    before = jnp.cumsum(route_hot, axis=0) - route_hot
    slot_index = jnp.sum(before * route_hot, axis=-1)
    target = (flat_routes * capacity + slot_index).reshape(rows, 2)
    slots = experts * capacity
    slot_ids = jnp.arange(slots, dtype=jnp.int32)
    place_first = slot_ids[:, None] == target[None, :, 0]
    place_second = slot_ids[:, None] == target[None, :, 1]
    place_any = jnp.logical_or(place_first, place_second).astype(low)

    shard_in = expert_in[0].astype(low).reshape(slab, 2, grps, QUAD, units)
    in_pieces = jnp.transpose(shard_in, (1, 3, 0, 2, 4)).reshape(2, 1, QUAD, slab, quarter)
    in_pieces = jnp.broadcast_to(in_pieces, (2, grps, QUAD, slab, quarter)).reshape(
        2, reps, slab, quarter
    )
    down_mine = spread(expert_out[0].astype(low), "grp").reshape(quarter, width)
    gate_mine = swap(in_pieces[0], REP).reshape(width, quarter)
    up_mine = swap(in_pieces[1], REP).reshape(width, quarter)

    upstream = my_cotangent.astype(full) * valid_rows[:, None]

    def to_experts(block):
        sent = block.reshape((1, experts) + block.shape[1:])
        sent = jnp.broadcast_to(sent, (QUAD,) + sent.shape[1:])
        return swap(sent.reshape((QUAD * experts,) + block.shape[1:]), PLANE)

    def dispatch(values):
        return dot(place_any, values).astype(low).reshape(experts, capacity, width)

    expert_upstream = to_experts(dispatch(upstream.astype(low))).reshape(-1, width)
    active_grad_bare = lax.dot_general(
        expert_upstream, down_mine, (((1,), (1,)), ((), ())), preferred_element_type=full
    )

    x_group = group_tokens.astype(full)
    scale_group = lax.rsqrt(jnp.mean(x_group * x_group, axis=-1, keepdims=True) + eps_norm)
    normed_group = (x_group * scale_group * gain_one).astype(low).reshape(exps * rows, width)
    qkv = dot(normed_group, qkv_mine).astype(low).reshape(exps, rows, 3, heads, head_dim)
    queries = qkv[:, :, 0]
    key_rows = qkv[:, :, 1]
    values = qkv[:, :, 2]
    onehot = bucket_onehot(rows)
    bias_mine = lax.dynamic_slice_in_dim(rel_bias, place * heads, heads, 1)
    bias_table = jnp.einsum("ijb,bh->hij", onehot, bias_mine, precision=highest)

    def scores_of():
        raw = (
            jnp.einsum("sihd,sjhd->shij", queries, key_rows, preferred_element_type=full)
            * score_scale
            + bias_table[None]
        )
        return jnp.where(key_ok[:, None, None, :], raw, -1e30)

    scores = scores_of()
    row_max = jnp.max(scores, axis=-1, keepdims=True)
    log_total = row_max + jnp.log(jnp.sum(jnp.exp(scores - row_max), axis=-1, keepdims=True))
    weights_low = jnp.exp(scores - log_total).astype(low)
    context_mine = (
        jnp.einsum("shij,sjhd->sihd", weights_low, values, preferred_element_type=full)
        .astype(low)
        .reshape(exps, rows, head_cols)
    )
    context = jnp.transpose(swap(context_mine, "exp"), (1, 0, 2)).reshape(rows, width)

    x_float = tokens.astype(full)
    scale_one = lax.rsqrt(jnp.mean(x_float * x_float, axis=-1, keepdims=True) + eps_norm)
    hidden_one = x_float + dot(context, full_out)
    scale_two = lax.rsqrt(jnp.mean(hidden_one * hidden_one, axis=-1, keepdims=True) + eps_norm)
    normed_two = (hidden_one * scale_two * gain_two).astype(low)
    normed_float = normed_two.astype(full)
    router_probs = jax.nn.softmax(jnp.dot(normed_float, router, precision=highest), axis=-1)
    picked = jnp.sum(router_probs[:, None, :] * chosen, axis=-1)
    gate_total = jnp.sum(picked, axis=-1, keepdims=True)
    gate_value = picked / gate_total
    combine = gate_value * valid_rows[:, None]
    combine_slots = jnp.sum(
        jnp.where(place_first, combine[None, :, 0], 0.0)
        + jnp.where(place_second, combine[None, :, 1], 0.0),
        axis=1,
    ).reshape(experts, 1, capacity)

    expert_rows = to_experts(dispatch(normed_two)).reshape(-1, width)
    expert_combine = to_experts(combine_slots).reshape(-1, 1)

    gate_part = dot(expert_rows, gate_mine)
    up_part = dot(expert_rows, up_mine)
    active_float, active_pull = jax.vjp(gated_unit, gate_part, up_part)
    active = active_float.astype(low)
    active_scaled = (active_float * expert_combine).astype(low)
    combine_grad_part = jnp.sum(active_float * active_grad_bare, axis=-1).reshape(
        QUAD * experts, 1, capacity
    )
    gate_part_grad, up_part_grad = active_pull(active_grad_bare * expert_combine)
    gate_part_grad = gate_part_grad.astype(low)
    up_part_grad = up_part_grad.astype(low)
    rows_grad_part = (
        lax.dot_general(gate_part_grad, gate_mine, (((1,), (1,)), ((), ())), preferred_element_type=full)
        + lax.dot_general(up_part_grad, up_mine, (((1,), (1,)), ((), ())), preferred_element_type=full)
    ).astype(low)
    output_part = dot(active, down_mine).astype(low)

    combine_grad_back = swap(combine_grad_part, PLANE)
    rows_grad_back = swap(rows_grad_part.reshape(QUAD * experts, capacity, width), PLANE)
    output_back = swap(output_part.reshape(QUAD * experts, capacity, width), PLANE)

    def transposed_dot(a, b):
        return lax.dot_general(a, b, (((0,), (0,)), ((), ())), preferred_element_type=full)

    down_grad = transposed_dot(active_scaled, expert_upstream).astype(low)
    gate_grad = transposed_dot(expert_rows, gate_part_grad).astype(low)
    up_grad = transposed_dot(expert_rows, up_part_grad).astype(low)
    down_share = jnp.sum(
        swap(down_grad.reshape(grps, units, width), "grp").astype(full), axis=0
    )[None]

    def in_columns(grad):
        back = swap(grad.reshape(reps, slab, quarter), REP).astype(full)
        back = jnp.sum(back.reshape(grps, QUAD, slab, grps, units), axis=0)
        return jnp.transpose(back, (1, 2, 0, 3)).reshape(slab, grps * QUAD * units)

    in_share = jnp.concatenate([in_columns(gate_grad), in_columns(up_grad)], axis=1)[None]

    def from_slots(placed, parts):
        hot = jnp.broadcast_to(placed.astype(low)[None], (QUAD,) + placed.shape).reshape(-1, rows)
        return lax.dot_general(
            hot, parts.reshape(-1, width), (((0,), (0,)), ((), ())), preferred_element_type=full
        )

    mixture = combine[:, :1] * from_slots(place_first, output_back) + combine[:, 1:] * from_slots(
        place_second, output_back
    )
    block_loader = (valid_rows[:, None] * (hidden_one + mixture)).astype(low)
    seq_ids = jnp.arange(deal.shape[0], dtype=jnp.int32)
    dealt_seq = jnp.sum(jnp.where(deal == me, seq_ids, 0))
    block_out = lax.dynamic_index_in_dim(
        spread(block_loader, "exp"), dealt_seq - base, 0, keepdims=False
    )

    combine_grad_slots = jnp.sum(combine_grad_back.reshape(QUAD, slots), axis=0)
    combine_grad = jnp.stack(
        [
            jnp.sum(jnp.where(place_first, combine_grad_slots[:, None], 0.0), axis=0),
            jnp.sum(jnp.where(place_second, combine_grad_slots[:, None], 0.0), axis=0),
        ],
        axis=1,
    )
    gate_grad_value = combine_grad * valid_rows[:, None]
    picked_grad = (
        gate_grad_value - jnp.sum(gate_grad_value * gate_value, axis=-1, keepdims=True)
    ) / gate_total
    probs_grad = jnp.sum(picked_grad[:, :, None] * chosen, axis=1)
    logit_grad = router_probs * (
        probs_grad - jnp.sum(probs_grad * router_probs, axis=-1, keepdims=True)
    )
    router_grad = jnp.dot(normed_float.T, logit_grad, precision=highest)
    normed_grad = jnp.dot(logit_grad, router.T, precision=highest) + from_slots(
        jnp.logical_or(place_first, place_second), rows_grad_back
    )
    scaled_two = normed_grad * gain_two
    hidden_grad = (
        upstream
        + scale_two * scaled_two
        - hidden_one * scale_two**3 * jnp.mean(scaled_two * hidden_one, axis=-1, keepdims=True)
    )
    gain_two_grad = jnp.sum(normed_grad * hidden_one * scale_two, axis=0)
    branch_grad = hidden_grad.astype(low)
    context_grad = lax.dot_general(
        branch_grad, full_out, (((1,), (1,)), ((), ())), preferred_element_type=full
    ).astype(low)
    context_grad_pieces = jnp.transpose(context_grad.reshape(rows, exps, head_cols), (1, 0, 2))
    context_grad_mine = swap(context_grad_pieces, "exp").reshape(exps, rows, heads, head_dim)
    branch_group = spread(branch_grad, "exp").reshape(exps * rows, width)
    out_grad = transposed_dot(context_mine.reshape(exps * rows, head_cols), branch_group).astype(low)

    scores = scores_of()
    probs_again = jnp.exp(scores - log_total)
    weights_again = probs_again.astype(low)
    values_grad = jnp.einsum(
        "shij,sihd->sjhd", weights_again, context_grad_mine, preferred_element_type=full
    )
    probs_grad_att = jnp.einsum(
        "sihd,sjhd->shij", context_grad_mine, values, preferred_element_type=full
    )
    row_delta = jnp.sum(probs_grad_att * probs_again, axis=-1, keepdims=True)
    scores_grad = (probs_again * (probs_grad_att - row_delta)).astype(low)
    scores_grad_sum = jnp.sum(scores_grad.astype(full), axis=0)
    bias_grad_mine = jnp.einsum("hij,ijb->bh", scores_grad_sum, onehot, precision=highest)
    bias_grad = lax.dynamic_update_slice_in_dim(
        jnp.zeros((BUCKETS, HEADS), full), bias_grad_mine, place * heads, 1
    )
    queries_grad = (
        jnp.einsum("shij,sjhd->sihd", scores_grad, key_rows, preferred_element_type=full)
        * score_scale
    )
    keys_grad = (
        jnp.einsum("shij,sihd->sjhd", scores_grad, queries, preferred_element_type=full)
        * score_scale
    )
    qkv_grad = (
        jnp.stack([queries_grad, keys_grad, values_grad], axis=2)
        .astype(low)
        .reshape(exps * rows, 3 * head_cols)
    )
    normed_one_part = lax.dot_general(
        qkv_grad, qkv_mine, (((1,), (1,)), ((), ())), preferred_element_type=full
    ).astype(low)
    normed_one_grad = jnp.sum(
        swap(normed_one_part.reshape(exps, rows, width), "exp").astype(full), axis=0
    )
    scaled_one = normed_one_grad * gain_one
    token_grad = (
        hidden_grad
        + scale_one * scaled_one
        - x_float * scale_one**3 * jnp.mean(scaled_one * x_float, axis=-1, keepdims=True)
    )
    gain_one_grad = jnp.sum(normed_one_grad * x_float * scale_one, axis=0)

    qkv_weight_grad = transposed_dot(normed_group, qkv_grad).astype(low)
    qkv_grad_rows = swap(qkv_weight_grad.reshape(exps, row_block, 3 * head_cols), "exp")
    qkv_grad_rows = jnp.transpose(
        qkv_grad_rows.reshape(exps, row_block, 3, head_cols), (1, 2, 0, 3)
    ).reshape(row_block, reps, -1)
    qkv_share = jnp.sum(
        swap(jnp.transpose(qkv_grad_rows, (1, 0, 2)), REP).astype(full), axis=0
    )
    out_pieces = jnp.transpose(out_grad.reshape(row_block, reps, -1), (1, 0, 2))
    out_share = jnp.sum(swap(out_pieces, REP).astype(full), axis=0)

    small = jnp.concatenate(
        [
            router_grad.reshape(-1),
            jnp.stack([gain_one_grad, gain_two_grad], axis=1).reshape(-1),
            bias_grad.reshape(-1),
        ]
    ).reshape(-1, 128)
    small_total = jnp.sum(lax.all_gather(small, ALL, axis=0, tiled=False), axis=0).reshape(-1)
    router_total = small_total[: router.size].reshape(router.shape)
    gains_total = small_total[router.size : router.size + norm_gains.size].reshape(norm_gains.shape)
    bias_total = small_total[router.size + norm_gains.size :].reshape(rel_bias.shape)

    qkv_new = adamw_update(attn_qkv, qkv_first, qkv_second, qkv_share, 1.5 / math.sqrt(D), 0.1)
    out_new = adamw_update(attn_out, out_first, out_second, out_share, 6.0 / math.sqrt(D), 0.1)
    bias_new = adamw_update(rel_bias, bias_first, bias_second, bias_total, 0.3, 0.0)
    router_new = adamw_update(
        router, router_first, router_second, router_total, 1.0 / math.sqrt(D), 0.1
    )
    gains_new = adamw_update(norm_gains, gains_first, gains_second, gains_total, 0.5, 0.0)
    in_new = adamw_update(expert_in, in_first, in_second, in_share, 1.5 / math.sqrt(D), 0.1)
    down_new = adamw_update(
        expert_out, down_first, down_second, down_share, 1.5 / math.sqrt(FF), 0.1
    )
    return (
        (block_out, token_grad)
        + qkv_new
        + out_new
        + bias_new
        + router_new
        + gains_new
        + in_new
        + down_new
    )


def solution(mesh):
    reps, exps = mesh.devices.shape
    split = Mesh(mesh.devices.reshape(reps // QUAD, QUAD, exps), ALL)
    by_rows = P(ALL, None)
    attn = P("exp", REP)
    expert = P("exp", REP, None)
    return jax.shard_map(
        per_device if QUAD * exps <= 16 else plain_device,
        mesh=split,
        in_specs=(by_rows, by_rows) + (P(),) * 3 + (attn,) * 6 + (P(),) * 9 + (expert,) * 6,
        out_specs=(by_rows, by_rows) + (attn,) * 6 + (P(),) * 9 + (expert,) * 6,
        check_vma=False,
    )
```

```python
import functools
import math

import jax
import jax.numpy as jnp
from jax import lax
from jax.experimental import pallas as pl
from jax.experimental.pallas import tpu as pltpu
from jax.sharding import Mesh
from jax.sharding import PartitionSpec as P

D = 1024
HEADS = 16
FF = 2816
BUCKETS = 32
STEP = 10
QUAD = 4
REP = ("grp", "quad")
PLANE = ("quad", "exp")
ALL = ("grp", "quad", "exp")

highest = lax.Precision.HIGHEST
eps_norm = 1e-06
thresholds = (1, 2, 3, 4, 5, 6, 7, 8, 11, 16, 22, 32, 45, 64, 90)
beta_one = 0.9
beta_two = 0.999
eps_adam = 1e-08
low = jnp.bfloat16
full = jnp.float32
MESH = pl.DeviceIdType.MESH


def adamw_update(weight, moment, second, gradient, step_rate, decay_factor):
    new_moment = beta_one * moment + (1.0 - beta_one) * gradient
    new_second = beta_two * second + (1.0 - beta_two) * gradient * gradient
    corrected = new_moment / (1.0 - beta_one**STEP)
    scaled = new_second / (1.0 - beta_two**STEP)
    new_weight = weight - step_rate * (
        corrected / (jnp.sqrt(scaled) + eps_adam) + decay_factor * weight
    )
    return (new_moment, new_second, new_weight)


def gated_unit(gate_input, up_input):
    return jax.nn.gelu(gate_input, approximate=True) * up_input


def dot(a, b):
    return jnp.dot(a, b, preferred_element_type=full)


def nt(a, b, precision=None):
    return lax.dot_general(a, b, (((1,), (1,)), ((), ())), preferred_element_type=full, precision=precision)


def tn(a, b):
    return lax.dot_general(a, b, (((0,), (0,)), ((), ())), preferred_element_type=full)


class Where:
    def __init__(self, grps, exps):
        self.grps, self.exps = grps, exps
        self.reps = grps * QUAD
        self.grp = lax.axis_index("grp")
        self.quad = lax.axis_index("quad")
        self.exp = lax.axis_index("exp")
        self.rep = self.grp * QUAD + self.quad
        self.base = self.rep * exps
        self.me = self.base + self.exp

    def device(self, rep, exp):
        return (rep // QUAD, rep % QUAD, exp)

    def near(self, flip):
        q = self.quad
        if flip & 1:
            q = q + 1 - 2 * (q % 2)
        if flip & 2:
            q = q + 2 - 4 * (q // 2)
        return q


def send(src, dst, send_sem, recv_sem, device):
    return pltpu.make_async_remote_copy(
        src_ref=src, dst_ref=dst, send_sem=send_sem, recv_sem=recv_sem, device_id=device, device_id_type=MESH
    )


def arrived(ref, sem):
    pltpu.make_async_copy(ref, ref, sem).wait()


def greet_all(at):
    count = at.reps * at.exps
    barrier = pltpu.get_barrier_semaphore()

    def greet(k, _):
        other = (at.me + k) % count
        pl.semaphore_signal(
            barrier, inc=1, device_id=at.device(other // at.exps, other % at.exps), device_id_type=MESH
        )
        return 0

    lax.fori_loop(1, count, greet, 0)
    pl.semaphore_wait(barrier, count - 1)


def lane_of(shape):
    return lax.broadcasted_iota(jnp.int32, shape, 1)


def row_of(shape):
    return lax.broadcasted_iota(jnp.int32, shape, 0)


def bucket_of(offset):
    distance = jnp.abs(offset)
    bucket = jnp.where(offset > 0, 16, 0)
    for threshold in thresholds:
        bucket = bucket + jnp.where(distance >= threshold, 1, 0)
    return bucket


def bits_of(count):
    return count.bit_length() - 1


def column_parts(width):
    tiles = width // 128
    cuts = [0, (tiles + 2) // 3, (2 * tiles + 2) // 3, tiles]
    return [(cuts[i] * 128, (cuts[i + 1] - cuts[i]) * 128) for i in range(3)]


def flipped(place, bit):
    return place + (1 - 2 * ((place // (1 << bit)) % 2)) * (1 << bit)


class Doubling:
    def __init__(self, at, own, every, sems, core_sems, orders):
        self.at, self.own, self.every = at, own, every
        self.sems, self.core_sems, self.orders = sems, core_sems, orders
        self.plane = at.quad * at.exps + at.exp
        self.steps = len(orders[0])
        self.parts = column_parts(own.shape[1])

    def device(self, bit):
        other = flipped(self.plane, bit)
        return (self.at.grp, other // self.at.exps, other % self.at.exps)

    def place(self, part, j):
        p = self.plane
        for i, bit in enumerate(self.orders[part]):
            if (j >> i) & 1:
                p = flipped(p, bit + 1)
        return p

    def block(self, part, p):
        begin, size = self.parts[part]
        return self.every.at[p, :, pl.ds(begin, size)]

    def source(self, part, j):
        begin, size = self.parts[part]
        return self.own.at[:, pl.ds(begin, size)] if j == 0 else self.block(part, self.place(part, j))

    def index(self, step, part, j):
        return part * (1 << self.steps) + (1 << step) - 1 + j

    def copy(self, step, part, j):
        i = self.index(step, part, j)
        return send(
            self.source(part, j),
            self.block(part, self.place(part, j)),
            self.sems.at[0, i],
            self.sems.at[1, i],
            self.device(self.orders[part][step] + 1),
        )

    def core_copy(self, part, j):
        i = part * (1 << self.steps) + j
        return send(
            self.source(part, j),
            self.block(part, self.place(part, j)),
            self.core_sems.at[0, i],
            self.core_sems.at[1, i],
            self.device(0),
        )

    def start(self):
        for part in range(3):
            for step in range(self.steps):
                self.copy(step, part, 0).start()
        for part in range(3):
            self.core_copy(part, 0).start()
        self.keep().start()

    def keep(self):
        return pltpu.make_async_copy(self.own, self.every.at[self.plane], self.core_sems.at[1, 3 << self.steps])

    def next(self, step):
        for part in range(3):
            for j in range(1 << step):
                k = (1 << step) + j
                arrived(self.block(part, self.place(part, k)), self.sems.at[1, self.index(step, part, j)])
                for later in range(step + 1, self.steps):
                    self.copy(later, part, k).start()
                self.core_copy(part, k).start()

    def finish_in(self):
        for part in range(3):
            for j in range(1 << self.steps):
                there = self.block(part, flipped(self.place(part, j), 0))
                arrived(there, self.core_sems.at[1, part * (1 << self.steps) + j])
        self.keep().wait()

    def finish_out(self):
        for part in range(3):
            for j in range(1 << self.steps):
                self.core_copy(part, j).wait_send()
            for step in range(self.steps):
                for j in range(1 << step):
                    self.copy(step, part, j).wait_send()


class Tiles:
    def __init__(self, units, reps):
        self.units = units
        self.half = units * reps // 256
        self.wide = (self.half + 1) // 2
        self.size = 128 * self.wide

    def start(self, quad):
        return 128 * (self.half * (quad // 2) + (self.half - self.wide) * (quad % 2))

    def rows(self):
        edge = 128 * self.wide
        first = 128 * (self.half - self.wide)
        result = []
        for k in range(QUAD):
            begin, end = k * self.units, (k + 1) * self.units
            pieces = []
            if begin < edge:
                pieces.append((0, min(end, edge) - begin, 0, begin))
            if end > edge:
                low_row = max(begin, edge)
                pieces.append((low_row - begin, end - low_row, 1, low_row - first))
            result.append(pieces)
        return result


def forward_kernel(
    grps,
    exps,
    lengths,
    rel_bias,
    routes_col,
    tokens,
    cotangent,
    gains,
    router,
    qkv_t,
    out_w,
    in_low,
    down_slab,
    gate_w,
    up_w,
    down_w,
    cot_all,
    n_all,
    comb_all,
    qkv_out,
    lse_out,
    mine_out,
    n1_out,
    wqkv_out,
    wout_out,
    h1_out,
    n2_out,
    probs_out,
    tok_all,
    wqkv,
    wout,
    n1,
    qkv,
    lse,
    mine,
    ctx,
    bias,
    comb_send,
    nothing,
    tok_sem,
    wq_sem,
    wo_sem,
    wo2_sem,
    weight_sem,
    weight2_sem,
    down_sem,
    ctx_sem,
    cot_sem,
    cot_core_sem,
    n_sem,
    n_core_sem,
    comb_sem,
    store_sem,
):
    at = Where(grps, exps)
    reps = at.reps
    rows, width = tokens.shape
    heads = HEADS // exps
    head_dim = width // HEADS
    head_cols = heads * head_dim
    block_cols = min(128, head_cols)
    shard_cols, row_block = qkv_t.shape
    seg = math.gcd(shard_cols, head_cols)
    segs = shard_cols // seg
    slab = in_low.shape[0]
    hidden = in_low.shape[1] // 2
    tiles = Tiles(down_slab.shape[0], reps)
    plane = at.quad * exps + at.exp
    members = QUAD * exps
    scale = 1.0 / math.sqrt(head_dim)
    SEND, RECV = 0, 1

    greet_all(at)

    def exp_peer(k):
        return (at.exp + k) % exps

    for k in range(1, exps):
        peer = exp_peer(k)
        send(
            tokens, tok_all.at[at.exp], tok_sem.at[SEND, peer], tok_sem.at[RECV, at.exp], at.device(at.rep, peer)
        ).start()
    tok_all[at.exp] = tokens[...]

    def segment(k):
        col = (at.rep * segs + k) * seg
        section = col // width
        within = col - section * width
        owner = within // head_cols
        return owner, section * head_cols + within - owner * head_cols

    def segment_copy(k, shift):
        owner, offset = segment(k)
        src = qkv_t.at[pl.ds(k * seg, seg)]
        dst = wqkv.at[at.exp, pl.ds(pl.multiple_of(offset, seg), seg)]
        target = at.device((at.rep + shift) % reps, owner)
        return owner, src, dst, send(
            src, dst, wq_sem.at[SEND, k * reps + shift], wq_sem.at[RECV, at.exp * 3 * (head_cols // seg) + offset // seg], target
        )

    def over_segments(act, act_local):
        def one(i, _):
            k, shift = i // reps, i % reps
            owner, src, dst, copy = segment_copy(k, shift)
            stays = jnp.logical_and(shift == 0, owner == at.exp)

            @pl.when(jnp.logical_not(stays))
            def _():
                act(copy)

            @pl.when(stays)
            def _():
                act_local(k, src, dst)

            return 0

        lax.fori_loop(0, segs * reps, one, 0)

    def local_segment(k, src, dst):
        _, offset = segment(k)
        pltpu.make_async_copy(src, dst, wq_sem.at[RECV, at.exp * 3 * (head_cols // seg) + offset // seg]).start()

    over_segments(lambda copy: copy.start(), local_segment)

    for k in range(1, reps):
        other = (at.rep + k) % reps
        send(
            out_w, wout.at[at.exp, at.rep], wo_sem.at[SEND, other], wo_sem.at[RECV, at.rep], at.device(other, at.exp)
        ).start()
    wout[at.exp, at.rep] = out_w[...]
    chip_bits = list(range(bits_of(members) - 1))
    cots = Doubling(at, cotangent, cot_all, cot_sem, cot_core_sem, [chip_bits[::-1]] * 3)
    cots.start()

    span = 2 * rows
    bucket = bucket_of(lane_of((8, span)) - rows)
    for h in range(heads):
        line = jnp.zeros((8, span), full)
        for b in range(BUCKETS):
            line = jnp.where(bucket == b, rel_bias[b, at.exp * heads + h], line)
        whole = jnp.broadcast_to(line[0:1], (rows, span))
        bias[h] = pltpu.roll(whole, 0, 1, stride=1, stride_axis=0)[:, rows:]

    def norm_group(s, _):
        @pl.when(s != at.exp)
        def _():
            arrived(tok_all.at[s], tok_sem.at[RECV, s])

        x = tok_all[s].astype(full)
        r = lax.rsqrt(jnp.mean(x * x, axis=1, keepdims=True) + eps_norm)
        n1[s] = (x * r * gains[0:1, :]).astype(low)
        return 0

    lax.fori_loop(0, exps, norm_group, 0)

    here = pl.ds(pl.multiple_of(at.rep * slab, slab), slab)

    def columns(quad, section):
        return in_low.at[:, pl.ds(pl.multiple_of(section * hidden + tiles.start(quad), 128), tiles.size)]

    def weight_copies(k):
        other = (at.rep + k) % reps
        device = at.device(other, at.exp)
        return [
            send(
                columns(other % QUAD, 0), gate_w.at[here], weight_sem.at[SEND, other], weight_sem.at[RECV, at.rep], device
            ),
            send(
                columns(other % QUAD, 1), up_w.at[here], weight2_sem.at[SEND, other], weight2_sem.at[RECV, at.rep], device
            ),
        ]

    def own_weights():
        return [
            pltpu.make_async_copy(columns(at.quad, 0), gate_w.at[here], weight_sem.at[RECV, at.rep]),
            pltpu.make_async_copy(columns(at.quad, 1), up_w.at[here], weight2_sem.at[RECV, at.rep]),
        ]

    def over_down(act, act_local):
        for k, pieces in enumerate(tiles.rows()):
            for i, (begin, count, parity, to) in enumerate(pieces):
                quad = 2 * (at.rep // QUAD) + parity
                for g in range(grps):
                    src, dst = down_slab.at[pl.ds(begin, count)], down_w.at[pl.ds(to, count)]
                    stays = jnp.logical_and(at.grp == g, at.quad == quad)
                    mine_place = at.rep % QUAD == k

                    @pl.when(jnp.logical_and(mine_place, jnp.logical_not(stays)))
                    def _():
                        act(
                            functools.partial(
                                send, src, dst, down_sem.at[SEND, i * grps + g], down_sem.at[RECV, at.rep], (g, quad, at.exp)
                            )
                        )

                    @pl.when(jnp.logical_and(mine_place, stays))
                    def _():
                        act_local(functools.partial(pltpu.make_async_copy, src, dst, down_sem.at[RECV, at.rep]))

    def down_in():
        for parity in range(2):

            @pl.when(at.quad % 2 == parity)
            def _():
                for k, pieces in enumerate(tiles.rows()):
                    for begin, count, owner, to in pieces:
                        if owner == parity:
                            source = QUAD * (at.quad // 2) + k
                            arrived(down_w.at[pl.ds(to, count)], down_sem.at[RECV, source])

        @pl.when(at.quad % 2 == 1)
        def _():
            blank().wait()

    def blank():
        return pltpu.make_async_copy(nothing, down_w.at[pl.ds(0, nothing.shape[0])], down_sem.at[RECV, reps])

    nothing[...] = jnp.zeros_like(nothing)

    @pl.when(at.quad % 2 == 1)
    def _():
        blank().start()

    def start_weights(k, _):
        for copy in weight_copies(k):
            copy.start()
        return 0

    over_down(lambda copy: copy().start(), lambda copy: copy().start())
    for copy in own_weights():
        copy.start()
    lax.fori_loop(1, reps // 2 + 1, start_weights, 0)

    def wait_segment(i, _):
        e, j = i // (3 * head_cols // seg), i % (3 * head_cols // seg)
        arrived(wqkv.at[e, pl.ds(pl.multiple_of(j * seg, seg), seg)], wq_sem.at[RECV, i])
        return 0

    lax.fori_loop(0, exps * 3 * head_cols // seg, wait_segment, 0)

    def project(s, _):
        total = jnp.zeros((rows, 3 * head_cols), full)
        for e in range(exps):
            total = total + nt(n1[s, :, e * row_block : (e + 1) * row_block], wqkv[e])
        qkv[s] = total.astype(low)
        return 0

    lax.fori_loop(0, exps, project, 0)

    for k in range(1, reps):
        other = (at.rep + k) % reps
        arrived(wout.at[at.exp, other], wo_sem.at[RECV, other])

    def wout_copies():
        return [
            send(
                wout.at[at.exp],
                wout.at[at.exp],
                wo2_sem.at[SEND, exp_peer(k)],
                wo2_sem.at[RECV, at.exp],
                at.device(at.rep, exp_peer(k)),
            )
            for k in range(1, exps)
        ]

    for copy in wout_copies():
        copy.start()

    cots.next(0)

    def attend(i, _):
        s = (at.exp + 1 + i) % exps
        ok = lane_of((rows, rows)) < lengths[at.base + s]
        lane = lane_of((rows, block_cols))
        sums = jnp.zeros((rows, 128), full)
        for c in range(head_cols // block_cols):
            cols = slice(c * block_cols, (c + 1) * block_cols)
            q = qkv[s, :, cols]
            k = qkv[s, :, head_cols + c * block_cols : head_cols + (c + 1) * block_cols]
            v = qkv[s, :, 2 * head_cols + c * block_cols : 2 * head_cols + (c + 1) * block_cols]
            result = jnp.zeros((rows, block_cols), full)
            for t in range(block_cols // head_dim):
                h = c * (block_cols // head_dim) + t
                here = jnp.logical_and(lane >= t * head_dim, lane < (t + 1) * head_dim)
                scores = nt(jnp.where(here, q, jnp.zeros_like(q)), k) * scale + bias[h]
                scores = jnp.where(ok, scores, -1e30)
                top = jnp.max(scores, axis=1, keepdims=True)
                weights = jnp.exp(scores - top)
                total = jnp.sum(weights, axis=1, keepdims=True)
                weights = (weights * (1.0 / total)).astype(low)
                result = jnp.where(here, jnp.dot(weights, v, preferred_element_type=full), result)
                sums = jnp.where(lane_of((rows, 128)) == h, top + jnp.log(total), sums)
            mine[s, :, cols] = result.astype(low)
        lse[s] = sums

        @pl.when(i < exps - 1)
        def _():
            send(
                mine.at[s], ctx.at[at.exp], ctx_sem.at[SEND, s], ctx_sem.at[RECV, at.exp], at.device(at.rep, s)
            ).start()

        @pl.when(i == exps - 1)
        def _():
            pltpu.make_async_copy(mine.at[s], ctx.at[at.exp], ctx_sem.at[RECV, at.exp]).start()

        return 0

    lax.fori_loop(0, exps, attend, 0)

    cots.next(1)
    for k in range(1, exps):
        arrived(wout.at[exp_peer(k)], wo2_sem.at[RECV, exp_peer(k)])
    for e in range(exps):
        arrived(ctx.at[e], ctx_sem.at[RECV, e])

    out_cols = wout.shape[3]
    for r in range(reps):
        cols = slice(r * out_cols, (r + 1) * out_cols)
        total = tokens[:, cols].astype(full)
        for e in range(exps):
            total = total + jnp.dot(ctx[e], wout[e, r], preferred_element_type=full)
        h1_out[:, cols] = total
    h1 = h1_out[...]
    r2 = lax.rsqrt(jnp.mean(h1 * h1, axis=1, keepdims=True) + eps_norm)
    n2 = (h1 * r2 * gains[1:2, :]).astype(low)
    n2_out[...] = n2
    rotated = [chip_bits[c:] + chip_bits[:c] for c in range(3)]
    rows_two = Doubling(at, n2_out, n_all, n_sem, n_core_sem, rotated)
    rows_two.start()
    lax.fori_loop(reps // 2 + 1, reps, start_weights, 0)

    logits = jnp.dot(n2.astype(full), router[...], precision=highest, preferred_element_type=full)
    lane = lane_of((rows, 128))
    logits = jnp.where(lane < exps, logits, -1e30)
    probs = jnp.exp(logits - jnp.max(logits, axis=1, keepdims=True))
    probs = probs / jnp.sum(probs, axis=1, keepdims=True)
    probs_out[...] = probs
    mine_hot = jnp.logical_or(lane == routes_col[:, 0:1], lane == routes_col[:, 1:2])
    picked = jnp.where(mine_hot, probs, 0.0)
    comb = picked / jnp.sum(picked, axis=1, keepdims=True)
    comb = jnp.where(row_of((rows, 1)) < lengths[at.me], comb, 0.0)
    comb_send[...] = comb.T[0 : comb_send.shape[0]]

    def comb_copy(k):
        other = (plane + k) % members
        return send(
            comb_send,
            comb_all.at[plane],
            comb_sem.at[SEND, other],
            comb_sem.at[RECV, plane],
            (at.grp, other // exps, other % exps),
        )

    def start_comb(k, _):
        comb_copy(k).start()
        return 0

    lax.fori_loop(1, members, start_comb, 0)
    pltpu.make_async_copy(comb_send, comb_all.at[plane], comb_sem.at[RECV, plane]).start()
    rows_two.next(0)

    stores = [
        (qkv, qkv_out),
        (lse, lse_out),
        (mine, mine_out),
        (n1, n1_out),
        (wqkv, wqkv_out),
        (wout, wout_out),
    ]
    for i, (src, dst) in enumerate(stores):
        pltpu.make_async_copy(src, dst, store_sem.at[i]).start()

    for step in range(1, rows_two.steps):
        rows_two.next(step)
    for step in range(2, cots.steps):
        cots.next(step)

    cots.finish_in()
    rows_two.finish_in()

    def comb_in(k, _):
        arrived(comb_all.at[k], comb_sem.at[RECV, k])
        return 0

    lax.fori_loop(0, members, comb_in, 0)
    down_in()

    def weights_in(r, _):
        there = pl.ds(pl.multiple_of(r * slab, slab), slab)
        arrived(gate_w.at[there], weight_sem.at[RECV, r])
        arrived(up_w.at[there], weight2_sem.at[RECV, r])
        return 0

    lax.fori_loop(0, reps, weights_in, 0)

    for k in range(1, exps):
        peer = exp_peer(k)
        arrived(tokens, tok_sem.at[SEND, peer])
        arrived(mine.at[peer], ctx_sem.at[SEND, peer])
    over_segments(lambda copy: copy.wait_send(), lambda k, src, dst: None)
    for k in range(1, reps):
        arrived(out_w, wo_sem.at[SEND, (at.rep + k) % reps])
    for copy in wout_copies():
        copy.wait_send()
    cots.finish_out()
    rows_two.finish_out()

    def sent_comb(k, _):
        comb_copy(k).wait_send()
        return 0

    lax.fori_loop(1, members, sent_comb, 0)
    over_down(lambda copy: copy().wait_send(), lambda copy: None)

    def sent_weights(k, _):
        for copy in weight_copies(k):
            copy.wait_send()
        return 0

    lax.fori_loop(1, reps, sent_weights, 0)
    for i, (src, dst) in enumerate(stores):
        pltpu.make_async_copy(src, dst, store_sem.at[i]).wait()


def forward_call(
    grps, exps, lengths, rel_bias, routes_col, tokens, cotangent, gains, router, qkv_t, out_w, in_low, down_slab
):
    reps = grps * QUAD
    rows, width = tokens.shape
    head_cols = width // exps
    row_block = qkv_t.shape[1]
    seg = math.gcd(qkv_t.shape[0], head_cols)
    segs = qkv_t.shape[0] // seg
    units = down_slab.shape[0]
    out_cols = out_w.shape[1]
    heads = HEADS // exps
    members = QUAD * exps
    wide = Tiles(units, reps).size
    shape = jax.ShapeDtypeStruct
    vmem = pl.BlockSpec(memory_space=pltpu.VMEM)
    smem = pl.BlockSpec(memory_space=pltpu.SMEM)
    hbm = pl.BlockSpec(memory_space=pl.ANY)
    results = [
        (shape((width, wide), low), hbm),
        (shape((width, wide), low), hbm),
        (shape((wide, width), low), hbm),
        (shape((members, rows, width), low), hbm),
        (shape((members, rows, width), low), hbm),
        (shape((members, 8, rows), full), hbm),
        (shape((exps, rows, 3 * head_cols), low), hbm),
        (shape((exps, rows, 128), full), hbm),
        (shape((exps, rows, head_cols), low), hbm),
        (shape((exps, rows, width), low), hbm),
        (shape((exps, 3 * head_cols, row_block), low), hbm),
        (shape((exps, reps, row_block, out_cols), low), hbm),
        (shape((rows, width), full), vmem),
        (shape((rows, width), low), vmem),
        (shape((rows, 128), full), vmem),
    ]
    dma = pltpu.SemaphoreType.DMA
    chips = members // 2
    return pl.pallas_call(
        functools.partial(forward_kernel, grps, exps),
        out_shape=[r[0] for r in results],
        in_specs=[smem] * 2 + [vmem] * 7 + [hbm] * 2,
        out_specs=[r[1] for r in results],
        scratch_shapes=[
            pltpu.VMEM((exps, rows, width), low),
            pltpu.VMEM((exps, 3 * head_cols, row_block), low),
            pltpu.VMEM((exps, reps, row_block, out_cols), low),
            pltpu.VMEM((exps, rows, width), low),
            pltpu.VMEM((exps, rows, 3 * head_cols), low),
            pltpu.VMEM((exps, rows, 128), full),
            pltpu.VMEM((exps, rows, head_cols), low),
            pltpu.VMEM((exps, rows, head_cols), low),
            pltpu.VMEM((heads, rows, rows), full),
            pltpu.VMEM((8, rows), full),
            pltpu.VMEM((128, width), low),
            dma((2, exps)),
            dma((2, max(segs * reps, exps * 3 * head_cols // seg))),
            dma((2, reps)),
            dma((2, exps)),
            dma((2, reps)),
            dma((2, reps)),
            dma((2, max(reps + 1, 2 * grps))),
            dma((2, exps)),
            dma((2, 3 * chips)),
            dma((2, 3 * chips + 1)),
            dma((2, 3 * chips)),
            dma((2, 3 * chips + 1)),
            dma((2, members)),
            dma((6,)),
        ],
        compiler_params=pltpu.CompilerParams(
            collective_id=0, has_side_effects=True, vmem_limit_bytes=60 * 1024 * 1024
        ),
        name="forward",
    )(lengths, rel_bias, routes_col, tokens, cotangent, gains, router, qkv_t, out_w, in_low, down_slab)


def expert_kernel(
    exps,
    cap,
    order,
    routes,
    n_block,
    *rest,
):
    g_blocks, rest = rest[:exps], rest[exps:]
    comb, gate_w, up_w, down_w, n_sum, y_sum, c_sum, n_rows, g_rows, gate_grad, up_grad, active = rest
    rows = n_block.shape[1]
    me = order[order.shape[0] - 1]

    hot = jnp.logical_or(routes[0, 0] == me, routes[0, 1] == me)
    hot_low = jnp.where(hot, 1.0, 0.0).astype(low)
    earlier = jnp.where(row_of((rows, rows)) < lane_of((rows, rows)), 1.0, 0.0).astype(low)
    before = dot(hot_low, earlier)
    slot = row_of((cap, rows)).astype(full)
    places = []
    shares = []
    for j in range(exps):
        inside = jnp.logical_and(slot == before[j : j + 1, :], hot_low[j : j + 1, :].astype(full) > 0.5)
        place = jnp.where(inside, 1.0, 0.0)
        places.append(place.astype(low))
        shares.append(jnp.sum(place * comb[j, pl.ds(me, 1), :], axis=1, keepdims=True))
        here = slice(j * cap, (j + 1) * cap)
        n_rows[here] = dot(places[j], n_block[j]).astype(low)
        g_rows[here] = dot(places[j], g_blocks[j][0]).astype(low)
    share = jnp.concatenate(shares, axis=0)

    gate_part = dot(n_rows[...], gate_w[...])
    up_part = dot(n_rows[...], up_w[...])
    grad = nt(g_rows[...], down_w[...])
    curve = math.sqrt(2.0 / math.pi)
    square = gate_part * gate_part
    bend = jnp.tanh(curve * gate_part * (1.0 + 0.044715 * square))
    half = 0.5 * (1.0 + bend)
    gelu = gate_part * half
    slope = half + (0.5 * curve) * gate_part * (1.0 - bend * bend) * (1.0 + (3 * 0.044715) * square)
    both = gelu * up_part
    value = jnp.sum(both * grad, axis=1, keepdims=True)
    grad = grad * share
    active[...] = (both * share).astype(low)
    gate_grad[...] = (grad * up_part * slope).astype(low)
    up_grad[...] = (grad * gelu).astype(low)
    y = dot(active[...], down_w[...]).astype(low)
    n_back = (nt(gate_grad[...], gate_w[...]) + nt(up_grad[...], up_w[...])).astype(low)
    for j in range(exps):
        here = slice(j * cap, (j + 1) * cap)
        y_sum[j] = tn(places[j], y[here]).astype(low)
        n_sum[j] = tn(places[j], n_back[here]).astype(low)
        line = jnp.sum(places[j].astype(full) * value[here], axis=0, keepdims=True)
        c_sum[j] = jnp.broadcast_to(line, (8, rows))


def expert_call(exps, cap, order, routes, n_all, cot_all, comb_all, gate_w, up_w, down_w):
    members, rows, width = n_all.shape
    wide = gate_w.shape[1]
    shape = jax.ShapeDtypeStruct

    def block(*dims):
        return pl.BlockSpec(dims, lambda i, order: (i,) + (0,) * (len(dims) - 1))

    def whole(*dims):
        return pl.BlockSpec(dims, lambda i, order: (0,) * len(dims), pipeline_mode=pl.Buffered(1))

    def chosen(j):
        return pl.BlockSpec((1, rows, width), lambda i, order: (order[i * exps + j], 0, 0))

    slots = exps * cap
    return pl.pallas_call(
        functools.partial(expert_kernel, exps, cap),
        grid_spec=pltpu.PrefetchScalarGridSpec(
            num_scalar_prefetch=1,
            grid=(QUAD,),
            in_specs=[block(1, 2, 8, rows), block(exps, rows, width)]
            + [chosen(j) for j in range(exps)]
            + [block(exps, 8, rows), whole(width, wide), whole(width, wide), whole(wide, width)],
            out_specs=[
                block(exps, rows, width),
                block(exps, rows, width),
                block(exps, 8, rows),
                block(slots, width),
                block(slots, width),
                block(slots, wide),
                block(slots, wide),
                block(slots, wide),
            ],
        ),
        out_shape=[
            shape((members, rows, width), low),
            shape((members, rows, width), low),
            shape((members, 8, rows), full),
            shape((QUAD * slots, width), low),
            shape((QUAD * slots, width), low),
            shape((QUAD * slots, wide), low),
            shape((QUAD * slots, wide), low),
            shape((QUAD * slots, wide), low),
        ],
        compiler_params=pltpu.CompilerParams(vmem_limit_bytes=60 * 1024 * 1024),
        name="experts",
    )(order, routes, n_all, *([cot_all] * exps), comb_all, gate_w, up_w, down_w)


class Halving:
    def __init__(self, at, source, kept, bufs, sems, load_sem):
        self.at, self.source, self.kept, self.bufs = at, source, kept, bufs
        self.sems, self.load_sem = sems, load_sem
        self.plane = at.quad * at.exps + at.exp
        self.places = bits_of(QUAD * at.exps)
        self.chip_bits = list(range(self.places - 1))
        self.parts = column_parts(source.shape[2])
        self.orders = [self.chip_bits[c:] + self.chip_bits[:c] for c in range(3)]

    def device(self, bit):
        other = flipped(self.plane, bit)
        return (self.at.grp, other // self.at.exps, other % self.at.exps)

    def first(self):
        core = self.plane % 2
        count = 1 << (self.places - 1)
        device = self.device(0)

        def copies(j):
            return send(
                self.source.at[2 * j + 1 - core], self.bufs[0].at[j], self.sems.at[0, 0, j], self.sems.at[0, 1, j], device
            )

        def load(j):
            return pltpu.make_async_copy(self.source.at[2 * j + core], self.kept.at[j], self.load_sem.at[j])

        return count, copies, load

    def start_first(self):
        count, copies, load = self.first()

        def one(j, _):
            copies(j).start()
            load(j).start()
            return 0

        lax.fori_loop(0, count, one, 0)

    def add_first(self):
        count, copies, load = self.first()

        def one(j, _):
            arrived(self.bufs[0].at[j], self.sems.at[0, 1, j])
            load(j).wait()
            self.bufs[0][j] = (self.bufs[0][j].astype(full) + self.kept[j].astype(full)).astype(low)
            return 0

        lax.fori_loop(0, count, one, 0)

    def hop(self, step, part):
        order = self.orders[part]
        bit = order[step]
        left = [b for b in self.chip_bits if b not in order[:step]]
        pos = left.index(bit)
        half = 1 << (len(left) - 1)
        mine = (self.plane // (1 << (bit + 1))) % 2
        device = self.device(bit + 1)
        begin, size = self.parts[part]
        cols = pl.ds(begin, size)
        base = self.base(step, part)

        def index(j, value):
            return (j >> pos) * (1 << (pos + 1)) + value * (1 << pos) + j % (1 << pos)

        pairs = []
        for j in range(half):
            copy = functools.partial(
                send,
                self.bufs[step].at[index(j, 1 - mine), :, cols],
                self.bufs[step + 1].at[j, :, cols],
                self.sems.at[1, 0, base + j],
                self.sems.at[1, 1, base + j],
                device,
            )
            pairs.append((copy, index(j, mine), j))
        return pairs, begin, size, base

    def base(self, step, part):
        n = len(self.chip_bits)
        return part * (1 << n) + sum(1 << (n - 1 - s) for s in range(step))

    def start(self, step, part=None):
        for p in range(3) if part is None else [part]:
            for copy, _, _ in self.hop(step, p)[0]:
                copy().start()

    def add(self, step, part):
        pairs, begin, size, base = self.hop(step, part)
        cols = pl.ds(begin, size)
        here, there = self.bufs[step], self.bufs[step + 1]
        for _, keep, j in pairs:
            arrived(there.at[j, :, cols], self.sems.at[1, 1, base + j])
            there[j, :, begin : begin + size] = (
                there[j, :, begin : begin + size].astype(full) + here[keep, :, begin : begin + size].astype(full)
            ).astype(low)

    def next(self, step):
        for p in range(3):
            self.add(step, p)
            if step + 1 < len(self.chip_bits):
                self.start(step + 1, p)

    def result(self):
        return self.bufs[len(self.chip_bits)]

    def finish(self):
        count, copies, _ = self.first()

        def one(j, _):
            copies(j).wait_send()
            return 0

        lax.fori_loop(0, count, one, 0)
        for step in range(len(self.chip_bits)):
            for p in range(3):
                for copy, _, _ in self.hop(step, p)[0]:
                    copy().wait_send()


def backward_kernel(
    grps,
    exps,
    lengths,
    deal,
    rel_bias,
    n_parts,
    y_parts,
    c_parts,
    gate_grad,
    up_grad,
    down_grad,
    n1_in,
    routes_col,
    tokens,
    gains,
    router,
    h1_in,
    n2_in,
    g_in,
    probs_in,
    qkv,
    lse,
    mine,
    wqkv,
    wout,
    token_grad,
    block_out,
    small_out,
    in_parts,
    down_parts,
    qkv_parts,
    out_parts,
    kept,
    n_bufs,
    y_bufs,
    c_in,
    dh1,
    dz_send,
    dz_all,
    do_send,
    do_in,
    bias,
    bias_sum,
    dqkv,
    dn1_send,
    dn1_in,
    n1,
    wq_send,
    og_send,
    blk_send,
    blk_in,
    small_send,
    small_exp,
    small_sum,
    small_rep,
    n_sem,
    y_sem,
    load_sem,
    c_sem,
    weight_sem,
    weight2_sem,
    down_sem,
    dz_sem,
    do_sem,
    dn1_sem,
    wq_sem,
    og_sem,
    blk_sem,
    small_sem,
    small2_sem,
    n1_sem,
):
    at = Where(grps, exps)
    reps = at.reps
    rows, width = tokens.shape
    heads = HEADS // exps
    head_dim = width // HEADS
    head_cols = heads * head_dim
    block_cols = min(128, head_cols)
    row_block = wqkv.shape[2]
    out_cols = wout.shape[3]
    slab = in_parts.shape[1]
    hidden = in_parts.shape[2] // 2
    tiles = Tiles(down_parts.shape[1], reps)
    scale = 1.0 / math.sqrt(head_dim)
    SEND, RECV = 0, 1
    plane = at.quad * exps + at.exp
    members = QUAD * exps

    def exp_peer(k):
        return (at.exp + k) % exps

    greet_all(at)

    dn = Halving(at, n_parts, kept, n_bufs, n_sem, load_sem.at[0])
    ys = Halving(at, y_parts, kept, y_bufs, y_sem, load_sem.at[1])
    dn.start_first()
    n1_copy = pltpu.make_async_copy(n1_in, n1, n1_sem)
    n1_copy.start()

    def c_copy(k):
        other = (plane + k) % members
        return other, send(
            c_parts.at[other],
            c_in.at[plane],
            c_sem.at[SEND, other],
            c_sem.at[RECV, plane],
            (at.grp, other // exps, other % exps),
        )

    def start_c(k, _):
        c_copy(k)[1].start()
        return 0

    lax.fori_loop(1, members, start_c, 0)
    pltpu.make_async_copy(c_parts.at[plane], c_in.at[plane], c_sem.at[RECV, plane]).start()

    span = 2 * rows
    bucket = bucket_of(lane_of((8, span)) - rows)
    for h in range(heads):
        line = jnp.zeros((8, span), full)
        for b in range(BUCKETS):
            line = jnp.where(bucket == b, rel_bias[b, at.exp * heads + h], line)
        whole = jnp.broadcast_to(line[0:1], (rows, span))
        bias[h] = pltpu.roll(whole, 0, 1, stride=1, stride_axis=0)[:, rows:]

    dn.add_first()
    dn.start(0)
    ys.start_first()

    def wait_c(k, _):
        arrived(c_in.at[k], c_sem.at[RECV, k])
        return 0

    lax.fori_loop(0, members, wait_c, 0)
    lane = lane_of((rows, 128))
    comb_rows = []
    for e in range(exps):
        total = c_in[e]
        for q in range(1, QUAD):
            total = total + c_in[q * exps + e]
        comb_rows.append(total[0:1, :])
    comb_rows.append(jnp.zeros((128 - exps, rows), full))
    comb_grad = jnp.concatenate(comb_rows, axis=0).T
    valid = row_of((rows, 1)) < lengths[at.me]
    probs = probs_in[...]
    hot = jnp.logical_or(lane == routes_col[:, 0:1], lane == routes_col[:, 1:2])
    picked = jnp.where(hot, probs, 0.0)
    total = jnp.sum(picked, axis=1, keepdims=True)
    gate = picked / total
    gate_grad_rows = jnp.where(valid, comb_grad, 0.0)
    spread_grad = jnp.sum(gate_grad_rows * gate, axis=1, keepdims=True)
    probs_grad = jnp.where(hot, (gate_grad_rows - spread_grad) / total, 0.0)
    logit_grad = probs * (probs_grad - jnp.sum(probs_grad * probs, axis=1, keepdims=True))
    n2 = n2_in[...].astype(full)
    router_rows = lax.dot_general(
        logit_grad, n2, (((0,), (0,)), ((), ())), preferred_element_type=full, precision=highest
    )
    small_rows = small_send.shape[0]
    small_send[...] = jnp.zeros_like(small_send)
    small_send[0:exps, :] = router_rows[0:exps, :]
    router_back = nt(logit_grad, router[...], precision=highest)
    h1 = h1_in[...]
    r2 = lax.rsqrt(jnp.mean(h1 * h1, axis=1, keepdims=True) + eps_norm)

    dn.next(0)
    ys.add_first()
    dn.next(1)
    steps = len(dn.chip_bits)
    for step in range(2, steps):
        dn.next(step)

    def columns(quad, parity, section):
        skip = 128 * (2 * tiles.wide - tiles.half) * parity
        to = section * hidden + tiles.start(quad) + skip
        to = to if isinstance(to, int) else pl.multiple_of(to, 128)
        return pl.ds(skip, tiles.size - skip), pl.ds(to, tiles.size - skip)

    def weight_copies(k, parity):
        other = (at.rep + k) % reps
        device = at.device(other, at.exp)
        there = pl.ds(pl.multiple_of(other * slab, slab), slab)
        result = []
        for section, (grad, sems) in enumerate(((gate_grad, weight_sem), (up_grad, weight2_sem))):
            src, dst = columns(at.quad, parity, section)
            result.append(
                functools.partial(
                    send,
                    grad.at[there, src],
                    in_parts.at[at.grp, :, dst],
                    sems.at[SEND, other],
                    sems.at[RECV, at.rep],
                    device,
                )
            )
        return result

    def own_weights(parity):
        there = pl.ds(pl.multiple_of(at.rep * slab, slab), slab)
        result = []
        for section, (grad, sems) in enumerate(((gate_grad, weight_sem), (up_grad, weight2_sem))):
            src, dst = columns(at.quad, parity, section)
            result.append(
                pltpu.make_async_copy(grad.at[there, src], in_parts.at[at.grp, :, dst], sems.at[RECV, at.rep])
            )
        return result

    def over_weights(act):
        for parity in range(2):

            @pl.when(at.quad % 2 == parity)
            def _():
                def one(k, _):
                    for copy in weight_copies(k, parity):
                        act(copy)
                    return 0

                lax.fori_loop(1, reps, one, 0)

    def start_own_weights():
        for parity in range(2):

            @pl.when(at.quad % 2 == parity)
            def _():
                for copy in own_weights(parity):
                    copy.start()

    def weights_in():
        for rep in range(reps):
            quad = rep % QUAD
            for section, sems in enumerate((weight_sem, weight2_sem)):
                _, dst = columns(quad, quad % 2, section)
                arrived(in_parts.at[rep // QUAD, :, dst], sems.at[RECV, rep])

    def over_down(act, act_local):
        for k, pieces in enumerate(tiles.rows()):
            for begin, count, parity, to in pieces:
                src, dst = down_grad.at[pl.ds(to, count)], down_parts.at[at.grp, pl.ds(begin, count)]
                recv = down_sem.at[RECV, 2 * at.grp + parity]
                stays = jnp.logical_and(at.grp == at.quad // 2, at.quad == k)
                ours = at.quad % 2 == parity

                @pl.when(jnp.logical_and(ours, jnp.logical_not(stays)))
                def _():
                    act(functools.partial(send, src, dst, down_sem.at[SEND, k], recv, (at.quad // 2, k, at.exp)))

                @pl.when(jnp.logical_and(ours, stays))
                def _():
                    act_local(functools.partial(pltpu.make_async_copy, src, dst, recv))

    def down_in():
        for k, pieces in enumerate(tiles.rows()):

            @pl.when(at.quad == k)
            def _():
                for g in range(grps):
                    for begin, count, parity, _ in pieces:
                        arrived(down_parts.at[g, pl.ds(begin, count)], down_sem.at[RECV, 2 * g + parity])

    n2_grad = router_back + dn.result()[0].astype(full)
    scaled = n2_grad * gains[1:2, :]
    hidden_grad = (
        g_in[...].astype(full)
        + r2 * scaled
        - h1 * (r2 * r2 * r2) * jnp.mean(scaled * h1, axis=1, keepdims=True)
    )
    dh1[...] = hidden_grad
    small_send[exps + 1 : exps + 2, :] = jnp.sum(n2_grad * h1 * r2, axis=0, keepdims=True)
    branch = hidden_grad.astype(low)
    dz_send[...] = branch
    for e in range(exps):
        total = jnp.zeros((rows, row_block), full)
        for r in range(reps):
            total = total + nt(branch[:, r * out_cols : (r + 1) * out_cols], wout[e, r])
        do_send[e] = total.astype(low)

    def do_copies():
        return [
            send(
                do_send.at[exp_peer(k)],
                do_in.at[at.exp],
                do_sem.at[SEND, exp_peer(k)],
                do_sem.at[RECV, at.exp],
                at.device(at.rep, exp_peer(k)),
            )
            for k in range(1, exps)
        ]

    for copy in do_copies():
        copy.start()
    pltpu.make_async_copy(do_send.at[at.exp], do_in.at[at.exp], do_sem.at[RECV, at.exp]).start()

    def dz_copies():
        return [
            send(
                dz_send,
                dz_all.at[at.exp],
                dz_sem.at[SEND, exp_peer(k)],
                dz_sem.at[RECV, at.exp],
                at.device(at.rep, exp_peer(k)),
            )
            for k in range(1, exps)
        ]

    for copy in dz_copies():
        copy.start()
    dz_all[at.exp] = branch
    over_down(lambda copy: copy().start(), lambda copy: copy().start())
    over_weights(lambda copy: copy().start())
    start_own_weights()
    ys.start(0)

    bias_sum[...] = jnp.zeros_like(bias_sum)

    def attend_back(i, _):
        s = (at.exp + 1 + i) % exps
        arrived(do_in.at[s], do_sem.at[RECV, s])
        ok = lane_of((rows, rows)) < lengths[at.base + s]
        block_lane = lane_of((rows, block_cols))
        for c in range(head_cols // block_cols):
            cols = slice(c * block_cols, (c + 1) * block_cols)
            k_cols = slice(head_cols + c * block_cols, head_cols + (c + 1) * block_cols)
            v_cols = slice(2 * head_cols + c * block_cols, 2 * head_cols + (c + 1) * block_cols)
            q = qkv[s, :, cols]
            k = qkv[s, :, k_cols]
            v = qkv[s, :, v_cols]
            do = do_in[s, :, cols]
            dq = jnp.zeros((rows, block_cols), full)
            dk = jnp.zeros((rows, block_cols), full)
            dv = jnp.zeros((rows, block_cols), full)
            for t in range(block_cols // head_dim):
                h = c * (block_cols // head_dim) + t
                here = jnp.logical_and(block_lane >= t * head_dim, block_lane < (t + 1) * head_dim)
                zero = jnp.zeros_like(q)
                q_h = jnp.where(here, q, zero)
                do_h = jnp.where(here, do, zero)
                scores = nt(q_h, k) * scale + bias[h]
                total = jnp.sum(jnp.where(lane == h, lse[s], 0.0), axis=1, keepdims=True)
                p = jnp.where(ok, jnp.exp(scores - total), 0.0)
                dp = nt(do_h, v)
                delta = jnp.sum(dp * p, axis=1, keepdims=True)
                ds = (p * (dp - delta)).astype(low)
                bias_sum[h] += ds.astype(full)
                dv = jnp.where(here, tn(p.astype(low), do), dv)
                dq = jnp.where(here, jnp.dot(ds, k, preferred_element_type=full), dq)
                dk = jnp.where(here, tn(ds, q), dk)
            dqkv[s, :, cols] = (dq * scale).astype(low)
            dqkv[s, :, k_cols] = (dk * scale).astype(low)
            dqkv[s, :, v_cols] = dv.astype(low)
        for e in range(exps):
            dn1_send[s, :, e * row_block : (e + 1) * row_block] = jnp.dot(
                dqkv[s], wqkv[e], preferred_element_type=full
            ).astype(low)

        @pl.when(i < exps - 1)
        def _():
            send(
                dn1_send.at[s], dn1_in.at[at.exp], dn1_sem.at[SEND, s], dn1_sem.at[RECV, at.exp], at.device(at.rep, s)
            ).start()

        @pl.when(i == exps - 1)
        def _():
            pltpu.make_async_copy(dn1_send.at[s], dn1_in.at[at.exp], dn1_sem.at[RECV, at.exp]).start()

        return 0

    lax.fori_loop(0, exps, attend_back, 0)

    n1_copy.wait()
    seg = wq_send.shape[2]
    segs = qkv_parts.shape[1]
    parts = wq_send.shape[1]
    for e in range(exps):
        total = jnp.zeros((3 * head_cols, row_block), full)
        for s in range(exps):
            total = total + tn(dqkv[s], n1[s, :, e * row_block : (e + 1) * row_block])
        for j in range(parts):
            wq_send[e, j] = total[j * seg : (j + 1) * seg].astype(low)

    def owner(j):
        section, within = j // (head_cols // seg), j % (head_cols // seg)
        col = section * width + at.exp * head_cols + within * seg
        block = col // seg
        return block // segs, block % segs

    def wq_copy(i):
        e, j = i // parts, i % parts
        rep, k = owner(j)
        dst = qkv_parts.at[at.rep, k]
        recv = wq_sem.at[RECV, at.rep * segs + k]
        stays = jnp.logical_and(rep == at.rep, e == at.exp)
        return (
            stays,
            functools.partial(send, wq_send.at[e, j], dst, wq_sem.at[SEND, i], recv, at.device(rep, e)),
            functools.partial(pltpu.make_async_copy, wq_send.at[e, j], dst, recv),
        )

    def start_wq(i, _):
        stays, away, local = wq_copy(i)

        @pl.when(stays)
        def _():
            local().start()

        @pl.when(jnp.logical_not(stays))
        def _():
            away().start()

        return 0

    lax.fori_loop(0, exps * parts, start_wq, 0)
    for k in range(1, exps):
        arrived(dz_all.at[exp_peer(k)], dz_sem.at[RECV, exp_peer(k)])
    for r in range(reps):
        total = jnp.zeros((head_cols, out_cols), full)
        for s in range(exps):
            total = total + tn(mine[s], dz_all[s, :, r * out_cols : (r + 1) * out_cols])
        og_send[r] = total.astype(low)

    def og_copies():
        return [
            send(
                og_send.at[(at.rep + k) % reps],
                out_parts.at[at.rep],
                og_sem.at[SEND, (at.rep + k) % reps],
                og_sem.at[RECV, at.rep],
                at.device((at.rep + k) % reps, at.exp),
            )
            for k in range(1, reps)
        ]

    for copy in og_copies():
        copy.start()
    pltpu.make_async_copy(og_send.at[at.rep], out_parts.at[at.rep], og_sem.at[RECV, at.rep]).start()

    line_lane = lane_of((8, 128))
    line_row = row_of((8, 128))
    bias_line = jnp.zeros((8, 128), full)
    flip = jnp.where(row_of((rows, rows)) + lane_of((rows, rows)) == rows - 1, 1.0, 0.0)
    turned_bucket = bucket_of(rows - 1 - lane_of((8, span)))
    for h in range(heads):
        flipped = jnp.dot(bias_sum[h], flip, precision=highest, preferred_element_type=full)
        square = jnp.concatenate([flipped, jnp.zeros((rows, rows), full)], axis=1)
        turned = pltpu.roll(square, 0, 1, stride=1, stride_axis=0)
        sums = jnp.broadcast_to(jnp.sum(turned, axis=0, keepdims=True), (8, span))
        for b in range(BUCKETS):
            value = jnp.sum(jnp.where(turned_bucket == b, sums, 0.0), axis=1, keepdims=True)
            bias_line = jnp.where(jnp.logical_and(line_row == h, line_lane == b), value, bias_line)
    for h in range(heads):
        small_send[exps + 2 : exps + 3, h * 128 : (h + 1) * 128] = bias_line[h : h + 1, :]

    ys.next(0)

    for e in range(exps):
        arrived(dn1_in.at[e], dn1_sem.at[RECV, e])
    n1_grad = dn1_in[0].astype(full)
    for e in range(1, exps):
        n1_grad = n1_grad + dn1_in[e].astype(full)
    x = tokens[...].astype(full)
    r1 = lax.rsqrt(jnp.mean(x * x, axis=1, keepdims=True) + eps_norm)
    scaled = n1_grad * gains[0:1, :]
    token_grad[...] = (
        dh1[...] + r1 * scaled - x * (r1 * r1 * r1) * jnp.mean(scaled * x, axis=1, keepdims=True)
    )
    small_send[exps : exps + 1, :] = jnp.sum(n1_grad * x * r1, axis=0, keepdims=True)

    def small_copies():
        return [
            send(
                small_send,
                small_exp.at[at.exp],
                small_sem.at[SEND, exp_peer(k)],
                small_sem.at[RECV, at.exp],
                at.device(at.rep, exp_peer(k)),
            )
            for k in range(1, exps)
        ]

    for copy in small_copies():
        copy.start()
    small_exp[at.exp] = small_send[...]
    for step in range(1, steps):
        ys.next(step)
    block = jnp.where(valid, h1_in[...] + ys.result()[0].astype(full), 0.0).astype(low)
    blk_send[...] = block

    def blk_copies():
        return [
            send(
                blk_send,
                blk_in.at[at.exp],
                blk_sem.at[SEND, exp_peer(k)],
                blk_sem.at[RECV, at.exp],
                at.device(at.rep, exp_peer(k)),
            )
            for k in range(1, exps)
        ]

    for copy in blk_copies():
        copy.start()
    blk_in[at.exp] = block
    for k in range(1, exps):
        arrived(small_exp.at[exp_peer(k)], small_sem.at[RECV, exp_peer(k)])
    total = small_exp[0]
    for e in range(1, exps):
        total = total + small_exp[e]
    small_sum[0] = total
    for e in range(exps):
        small_sum[0, exps + 3 + e : exps + 4 + e, :] = small_exp[e, exps + 2 : exps + 3, :]

    def small2_copies():
        return [
            send(
                small_sum.at[0],
                small_rep.at[at.rep],
                small2_sem.at[SEND, (at.rep + k) % reps],
                small2_sem.at[RECV, at.rep],
                at.device((at.rep + k) % reps, at.exp),
            )
            for k in range(1, reps)
        ]

    for copy in small2_copies():
        copy.start()
    small_rep[at.rep] = small_sum[0]
    for k in range(1, exps):
        arrived(blk_in.at[exp_peer(k)], blk_sem.at[RECV, exp_peer(k)])
    chosen = jnp.zeros((rows, width), full)
    for e in range(exps):
        chosen = jnp.where(deal[at.base + e] == at.me, blk_in[e].astype(full), chosen)
    block_out[...] = chosen.astype(low)
    for k in range(1, reps):
        arrived(small_rep.at[(at.rep + k) % reps], small2_sem.at[RECV, (at.rep + k) % reps])
    total = small_rep[0]
    for r in range(1, reps):
        total = total + small_rep[r]
    small_out[...] = total

    weights_in()
    down_in()
    for r in range(reps):
        arrived(out_parts.at[r], og_sem.at[RECV, r])

    def wq_in(i, _):
        arrived(qkv_parts.at[i // segs, i % segs], wq_sem.at[RECV, i])
        return 0

    lax.fori_loop(0, reps * segs, wq_in, 0)

    def sent_c(k, _):
        c_copy(k)[1].wait_send()
        return 0

    lax.fori_loop(1, members, sent_c, 0)
    dn.finish()
    ys.finish()

    over_weights(lambda copy: copy().wait_send())
    over_down(lambda copy: copy().wait_send(), lambda copy: None)

    def sent_wq(i, _):
        stays, away, _ = wq_copy(i)

        @pl.when(jnp.logical_not(stays))
        def _():
            away().wait_send()

        return 0

    lax.fori_loop(0, exps * parts, sent_wq, 0)
    for copies in (
        do_copies(),
        dz_copies(),
        og_copies(),
        small_copies(),
        blk_copies(),
        small2_copies(),
    ):
        for copy in copies:
            copy.wait_send()
    for k in range(1, exps):
        arrived(dn1_send.at[exp_peer(k)], dn1_sem.at[SEND, exp_peer(k)])


def backward_call(
    grps, exps, hidden, lengths, deal, rel_bias, n_parts, y_parts, c_parts, gate_grad, up_grad, down_grad, n1, routes_col,
    tokens, gains, router, h1, n2, g, probs, qkv, lse, mine, wqkv, wout
):
    reps = grps * QUAD
    rows, width = tokens.shape
    heads = HEADS // exps
    head_cols = width // exps
    row_block = wqkv.shape[2]
    out_cols = wout.shape[3]
    shard_cols = 3 * width // reps
    seg = math.gcd(shard_cols, head_cols)
    segs = shard_cols // seg
    parts = 3 * head_cols // seg
    slab = width // reps
    members = QUAD * exps
    chip_bits = bits_of(members) - 1
    small_rows = -(-(2 * exps + 3) // 8) * 8
    shape = jax.ShapeDtypeStruct
    vmem = pl.BlockSpec(memory_space=pltpu.VMEM)
    smem = pl.BlockSpec(memory_space=pltpu.SMEM)
    hbm = pl.BlockSpec(memory_space=pl.ANY)
    results = [
        (shape((rows, width), full), vmem),
        (shape((rows, width), low), vmem),
        (shape((small_rows, width), full), vmem),
        (shape((grps, slab, 2 * hidden), low), hbm),
        (shape((grps, hidden // reps, width), low), hbm),
        (shape((reps, segs, seg, row_block), low), hbm),
        (shape((reps, row_block, out_cols), low), hbm),
    ]
    dma = pltpu.SemaphoreType.DMA
    bufs = [pltpu.VMEM((1 << (chip_bits - s), rows, width), low) for s in range(chip_bits + 1)]
    return pl.pallas_call(
        functools.partial(backward_kernel, grps, exps),
        out_shape=[r[0] for r in results],
        in_specs=[smem] * 3 + [hbm] * 7 + [vmem] * 13,
        out_specs=[r[1] for r in results],
        scratch_shapes=[
            pltpu.VMEM((members // 2, rows, width), low),
            list(bufs),
            list(bufs),
            pltpu.VMEM((members, 8, rows), full),
            pltpu.VMEM((rows, width), full),
            pltpu.VMEM((rows, width), low),
            pltpu.VMEM((exps, rows, width), low),
            pltpu.VMEM((exps, rows, head_cols), low),
            pltpu.VMEM((exps, rows, head_cols), low),
            pltpu.VMEM((heads, rows, rows), full),
            pltpu.VMEM((heads, rows, rows), full),
            pltpu.VMEM((exps, rows, 3 * head_cols), low),
            pltpu.VMEM((exps, rows, width), low),
            pltpu.VMEM((exps, rows, width), low),
            pltpu.VMEM((exps, rows, width), low),
            pltpu.VMEM((exps, parts, seg, row_block), low),
            pltpu.VMEM((reps, row_block, out_cols), low),
            pltpu.VMEM((rows, width), low),
            pltpu.VMEM((exps, rows, width), low),
            pltpu.VMEM((small_rows, width), full),
            pltpu.VMEM((exps, small_rows, width), full),
            pltpu.VMEM((1, small_rows, width), full),
            pltpu.VMEM((reps, small_rows, width), full),
            dma((2, 2, 3 << chip_bits)),
            dma((2, 2, 3 << chip_bits)),
            dma((2, members // 2)),
            dma((2, members)),
            dma((2, reps)),
            dma((2, reps)),
            dma((2, max(QUAD, 2 * grps))),
            dma((2, exps)),
            dma((2, exps)),
            dma((2, exps)),
            dma((2, max(exps * parts, reps * segs))),
            dma((2, reps)),
            dma((2, exps)),
            dma((2, exps)),
            dma((2, reps)),
            dma,
        ],
        compiler_params=pltpu.CompilerParams(
            collective_id=1, has_side_effects=True, vmem_limit_bytes=60 * 1024 * 1024
        ),
        name="backward",
    )(
        lengths, deal, rel_bias, n_parts, y_parts, c_parts, gate_grad, up_grad, down_grad, n1, routes_col, tokens,
        gains, router, h1, n2, g, probs, qkv, lse, mine, wqkv, wout
    )


def per_device(
    tokens,
    cotangent,
    seq_lengths,
    deal,
    routes,
    attn_qkv,
    qkv_first,
    qkv_second,
    attn_out,
    out_first,
    out_second,
    rel_bias,
    bias_first,
    bias_second,
    router,
    router_first,
    router_second,
    norm_gains,
    gains_first,
    gains_second,
    expert_in,
    in_first,
    in_second,
    expert_out,
    down_first,
    down_second,
):
    rows, width = tokens.shape
    experts = router.shape[1]
    capacity = (10 * rows + 4 * experts - 1) // (4 * experts)
    exps = lax.axis_size("exp")
    grps = lax.axis_size("grp")
    heads = HEADS // exps
    place = lax.axis_index("exp")
    quad = lax.axis_index("quad")
    base = lax.axis_index(REP) * exps
    me = base + place
    row_block = attn_qkv.shape[0]
    hidden = expert_in.shape[2] // 2
    members = QUAD * exps

    my_routes = lax.dynamic_slice_in_dim(routes, me * rows, rows, 0)
    routes_col = jnp.zeros((rows, 128), jnp.int32).at[:, :2].set(my_routes)
    gains = jnp.zeros((8, width), full).at[:2].set(norm_gains.T)
    router_wide = jnp.zeros((width, 128), full).at[:, :experts].set(router)
    (
        gate_w, up_w, down_w, cot_all, n_all, comb_all, qkv, lse, context_mine, normed_group, wqkv, wout,
        hidden_one, normed_two, router_probs,
    ) = forward_call(
        grps, exps, seq_lengths, rel_bias, routes_col, tokens, cotangent, gains, router_wide,
        attn_qkv.astype(low).T, attn_out.astype(low), expert_in[0].astype(low), expert_out[0].astype(low),
    )

    plane_base = base - quad * exps
    plane_deal = lax.dynamic_slice_in_dim(deal, plane_base, members, 0) - plane_base
    order = jnp.concatenate([plane_deal, place[None].astype(jnp.int32)]).astype(jnp.int32)
    plane_routes = lax.dynamic_slice_in_dim(routes, plane_base * rows, members * rows, 0)
    plane_routes = jnp.transpose(plane_routes.reshape(QUAD, exps, rows, 2), (0, 3, 1, 2))
    plane_routes = jnp.pad(plane_routes, ((0, 0), (0, 0), (0, 8 - exps), (0, 0)), constant_values=-1)
    n_parts, y_parts, c_parts, n_rows, g_rows, gate_part_grad, up_part_grad, active = expert_call(
        exps, capacity, order, plane_routes, n_all, cot_all, comb_all, gate_w, up_w, down_w
    )
    valid_rows = jnp.arange(rows, dtype=jnp.int32) < seq_lengths[me]
    my_cotangent = lax.dynamic_index_in_dim(cot_all, deal[me] - plane_base, 0, keepdims=False)
    my_cotangent = jnp.where(valid_rows[:, None], my_cotangent, jnp.zeros_like(my_cotangent))
    down_grad = tn(active, g_rows).astype(low)
    gate_grad = tn(n_rows, gate_part_grad).astype(low)
    up_grad = tn(n_rows, up_part_grad).astype(low)
    token_grad, block_out, small, in_parts, down_parts, qkv_parts, out_parts = backward_call(
        grps, exps, hidden, seq_lengths, deal, rel_bias, n_parts, y_parts, c_parts, gate_grad, up_grad, down_grad,
        normed_group, routes_col, tokens, gains, router_wide, hidden_one, normed_two, my_cotangent, router_probs,
        qkv, lse, context_mine, wqkv, wout,
    )
    down_share = jnp.sum(down_parts.astype(full), axis=0)[None]
    in_share = jnp.sum(in_parts.astype(full), axis=0)[None]
    qkv_share = jnp.sum(qkv_parts.astype(full), axis=0).reshape(-1, row_block).T
    out_share = jnp.sum(out_parts.astype(full), axis=0)
    router_total = small[:experts].T
    gains_total = small[exps : exps + 2].T
    bias_total = jnp.transpose(
        small[exps + 3 : 2 * exps + 3, : heads * 128].reshape(exps, heads, 128)[:, :, :BUCKETS], (2, 0, 1)
    ).reshape(BUCKETS, HEADS)

    qkv_new = adamw_update(attn_qkv, qkv_first, qkv_second, qkv_share, 1.5 / math.sqrt(D), 0.1)
    out_new = adamw_update(attn_out, out_first, out_second, out_share, 6.0 / math.sqrt(D), 0.1)
    bias_new = adamw_update(rel_bias, bias_first, bias_second, bias_total, 0.3, 0.0)
    router_new = adamw_update(
        router, router_first, router_second, router_total, 1.0 / math.sqrt(D), 0.1
    )
    gains_new = adamw_update(norm_gains, gains_first, gains_second, gains_total, 0.5, 0.0)
    in_new = adamw_update(expert_in, in_first, in_second, in_share, 1.5 / math.sqrt(D), 0.1)
    down_new = adamw_update(
        expert_out, down_first, down_second, down_share, 1.5 / math.sqrt(FF), 0.1
    )
    return (
        (block_out, token_grad)
        + qkv_new
        + out_new
        + bias_new
        + router_new
        + gains_new
        + in_new
        + down_new
    )


def bucket_onehot(length):
    places = jnp.arange(length, dtype=jnp.int32)
    offset = places[None, :] - places[:, None]
    distance = jnp.abs(offset)
    bucket = 16 * (offset > 0).astype(jnp.int32)
    for threshold in thresholds:
        bucket = bucket + (distance >= threshold).astype(jnp.int32)
    return (bucket[:, :, None] == jnp.arange(BUCKETS, dtype=jnp.int32)[None, None, :]).astype(full)


def swap(pieces, axes):
    return lax.all_to_all(pieces, axes, split_axis=0, concat_axis=0, tiled=True)


def spread(block, axes):
    members = lax.axis_size(axes)
    return swap(jnp.broadcast_to(block[None], (members,) + block.shape), axes)


def plain_device(
    tokens,
    cotangent,
    seq_lengths,
    deal,
    routes,
    attn_qkv,
    qkv_first,
    qkv_second,
    attn_out,
    out_first,
    out_second,
    rel_bias,
    bias_first,
    bias_second,
    router,
    router_first,
    router_second,
    norm_gains,
    gains_first,
    gains_second,
    expert_in,
    in_first,
    in_second,
    expert_out,
    down_first,
    down_second,
):
    rows, width = tokens.shape
    head_dim = width // HEADS
    score_scale = 1.0 / math.sqrt(head_dim)
    experts = router.shape[1]
    capacity = (10 * rows + 4 * experts - 1) // (4 * experts)
    exps = lax.axis_size("exp")
    grps = lax.axis_size("grp")
    reps = grps * QUAD
    heads = HEADS // exps
    head_cols = heads * head_dim
    place = lax.axis_index("exp")
    base = lax.axis_index(REP) * exps
    me = base + place
    slab = expert_in.shape[1]
    units = expert_out.shape[1]
    quarter = grps * units

    row_block = attn_qkv.shape[0]
    qkv_rows = lax.all_gather(attn_qkv.astype(low), REP, axis=1, tiled=True)
    out_rows = lax.all_gather(attn_out.astype(low), REP, axis=1, tiled=True)
    qkv_pieces = jnp.transpose(
        qkv_rows.reshape(row_block, 3, exps, head_cols), (2, 0, 1, 3)
    ).reshape(exps, row_block, 3 * head_cols)
    qkv_mine = swap(qkv_pieces, "exp").reshape(width, 3 * head_cols)
    full_out = spread(out_rows, "exp").reshape(width, width)

    group_tokens = spread(tokens, "exp")
    group_cotangent = spread(cotangent, "exp")
    my_cotangent = lax.dynamic_index_in_dim(group_cotangent, deal[me] - base, 0, keepdims=False)

    my_routes = lax.dynamic_slice_in_dim(routes, me * rows, rows, 0)
    places = jnp.arange(rows, dtype=jnp.int32)
    valid_rows = (places < seq_lengths[me]).astype(full)
    group_lengths = lax.dynamic_slice_in_dim(seq_lengths, base, exps, 0)
    key_ok = places[None, :] < group_lengths[:, None]
    gain_one = norm_gains[:, 0]
    gain_two = norm_gains[:, 1]

    chosen = (my_routes[:, :, None] == jnp.arange(experts, dtype=jnp.int32)[None, None, :]).astype(full)
    flat_routes = my_routes.reshape(-1)
    route_hot = (flat_routes[:, None] == jnp.arange(experts, dtype=jnp.int32)[None, :]).astype(jnp.int32)
    before = jnp.cumsum(route_hot, axis=0) - route_hot
    slot_index = jnp.sum(before * route_hot, axis=-1)
    target = (flat_routes * capacity + slot_index).reshape(rows, 2)
    slots = experts * capacity
    slot_ids = jnp.arange(slots, dtype=jnp.int32)
    place_first = slot_ids[:, None] == target[None, :, 0]
    place_second = slot_ids[:, None] == target[None, :, 1]
    place_any = jnp.logical_or(place_first, place_second).astype(low)

    shard_in = expert_in[0].astype(low).reshape(slab, 2, grps, QUAD, units)
    in_pieces = jnp.transpose(shard_in, (1, 3, 0, 2, 4)).reshape(2, 1, QUAD, slab, quarter)
    in_pieces = jnp.broadcast_to(in_pieces, (2, grps, QUAD, slab, quarter)).reshape(
        2, reps, slab, quarter
    )
    down_mine = spread(expert_out[0].astype(low), "grp").reshape(quarter, width)
    gate_mine = swap(in_pieces[0], REP).reshape(width, quarter)
    up_mine = swap(in_pieces[1], REP).reshape(width, quarter)

    upstream = my_cotangent.astype(full) * valid_rows[:, None]

    def to_experts(block):
        sent = block.reshape((1, experts) + block.shape[1:])
        sent = jnp.broadcast_to(sent, (QUAD,) + sent.shape[1:])
        return swap(sent.reshape((QUAD * experts,) + block.shape[1:]), PLANE)

    def dispatch(values):
        return dot(place_any, values).astype(low).reshape(experts, capacity, width)

    expert_upstream = to_experts(dispatch(upstream.astype(low))).reshape(-1, width)
    active_grad_bare = lax.dot_general(
        expert_upstream, down_mine, (((1,), (1,)), ((), ())), preferred_element_type=full
    )

    x_group = group_tokens.astype(full)
    scale_group = lax.rsqrt(jnp.mean(x_group * x_group, axis=-1, keepdims=True) + eps_norm)
    normed_group = (x_group * scale_group * gain_one).astype(low).reshape(exps * rows, width)
    qkv = dot(normed_group, qkv_mine).astype(low).reshape(exps, rows, 3, heads, head_dim)
    queries = qkv[:, :, 0]
    key_rows = qkv[:, :, 1]
    values = qkv[:, :, 2]
    onehot = bucket_onehot(rows)
    bias_mine = lax.dynamic_slice_in_dim(rel_bias, place * heads, heads, 1)
    bias_table = jnp.einsum("ijb,bh->hij", onehot, bias_mine, precision=highest)

    def scores_of():
        raw = (
            jnp.einsum("sihd,sjhd->shij", queries, key_rows, preferred_element_type=full)
            * score_scale
            + bias_table[None]
        )
        return jnp.where(key_ok[:, None, None, :], raw, -1e30)

    scores = scores_of()
    row_max = jnp.max(scores, axis=-1, keepdims=True)
    log_total = row_max + jnp.log(jnp.sum(jnp.exp(scores - row_max), axis=-1, keepdims=True))
    weights_low = jnp.exp(scores - log_total).astype(low)
    context_mine = (
        jnp.einsum("shij,sjhd->sihd", weights_low, values, preferred_element_type=full)
        .astype(low)
        .reshape(exps, rows, head_cols)
    )
    context = jnp.transpose(swap(context_mine, "exp"), (1, 0, 2)).reshape(rows, width)

    x_float = tokens.astype(full)
    scale_one = lax.rsqrt(jnp.mean(x_float * x_float, axis=-1, keepdims=True) + eps_norm)
    hidden_one = x_float + dot(context, full_out)
    scale_two = lax.rsqrt(jnp.mean(hidden_one * hidden_one, axis=-1, keepdims=True) + eps_norm)
    normed_two = (hidden_one * scale_two * gain_two).astype(low)
    normed_float = normed_two.astype(full)
    router_probs = jax.nn.softmax(jnp.dot(normed_float, router, precision=highest), axis=-1)
    picked = jnp.sum(router_probs[:, None, :] * chosen, axis=-1)
    gate_total = jnp.sum(picked, axis=-1, keepdims=True)
    gate_value = picked / gate_total
    combine = gate_value * valid_rows[:, None]
    combine_slots = jnp.sum(
        jnp.where(place_first, combine[None, :, 0], 0.0)
        + jnp.where(place_second, combine[None, :, 1], 0.0),
        axis=1,
    ).reshape(experts, 1, capacity)

    expert_rows = to_experts(dispatch(normed_two)).reshape(-1, width)
    expert_combine = to_experts(combine_slots).reshape(-1, 1)

    gate_part = dot(expert_rows, gate_mine)
    up_part = dot(expert_rows, up_mine)
    active_float, active_pull = jax.vjp(gated_unit, gate_part, up_part)
    active = active_float.astype(low)
    active_scaled = (active_float * expert_combine).astype(low)
    combine_grad_part = jnp.sum(active_float * active_grad_bare, axis=-1).reshape(
        QUAD * experts, 1, capacity
    )
    gate_part_grad, up_part_grad = active_pull(active_grad_bare * expert_combine)
    gate_part_grad = gate_part_grad.astype(low)
    up_part_grad = up_part_grad.astype(low)
    rows_grad_part = (
        lax.dot_general(gate_part_grad, gate_mine, (((1,), (1,)), ((), ())), preferred_element_type=full)
        + lax.dot_general(up_part_grad, up_mine, (((1,), (1,)), ((), ())), preferred_element_type=full)
    ).astype(low)
    output_part = dot(active, down_mine).astype(low)

    combine_grad_back = swap(combine_grad_part, PLANE)
    rows_grad_back = swap(rows_grad_part.reshape(QUAD * experts, capacity, width), PLANE)
    output_back = swap(output_part.reshape(QUAD * experts, capacity, width), PLANE)

    def transposed_dot(a, b):
        return lax.dot_general(a, b, (((0,), (0,)), ((), ())), preferred_element_type=full)

    down_grad = transposed_dot(active_scaled, expert_upstream).astype(low)
    gate_grad = transposed_dot(expert_rows, gate_part_grad).astype(low)
    up_grad = transposed_dot(expert_rows, up_part_grad).astype(low)
    down_share = jnp.sum(
        swap(down_grad.reshape(grps, units, width), "grp").astype(full), axis=0
    )[None]

    def in_columns(grad):
        back = swap(grad.reshape(reps, slab, quarter), REP).astype(full)
        back = jnp.sum(back.reshape(grps, QUAD, slab, grps, units), axis=0)
        return jnp.transpose(back, (1, 2, 0, 3)).reshape(slab, grps * QUAD * units)

    in_share = jnp.concatenate([in_columns(gate_grad), in_columns(up_grad)], axis=1)[None]

    def from_slots(placed, parts):
        hot = jnp.broadcast_to(placed.astype(low)[None], (QUAD,) + placed.shape).reshape(-1, rows)
        return lax.dot_general(
            hot, parts.reshape(-1, width), (((0,), (0,)), ((), ())), preferred_element_type=full
        )

    mixture = combine[:, :1] * from_slots(place_first, output_back) + combine[:, 1:] * from_slots(
        place_second, output_back
    )
    block_loader = (valid_rows[:, None] * (hidden_one + mixture)).astype(low)
    seq_ids = jnp.arange(deal.shape[0], dtype=jnp.int32)
    dealt_seq = jnp.sum(jnp.where(deal == me, seq_ids, 0))
    block_out = lax.dynamic_index_in_dim(
        spread(block_loader, "exp"), dealt_seq - base, 0, keepdims=False
    )

    combine_grad_slots = jnp.sum(combine_grad_back.reshape(QUAD, slots), axis=0)
    combine_grad = jnp.stack(
        [
            jnp.sum(jnp.where(place_first, combine_grad_slots[:, None], 0.0), axis=0),
            jnp.sum(jnp.where(place_second, combine_grad_slots[:, None], 0.0), axis=0),
        ],
        axis=1,
    )
    gate_grad_value = combine_grad * valid_rows[:, None]
    picked_grad = (
        gate_grad_value - jnp.sum(gate_grad_value * gate_value, axis=-1, keepdims=True)
    ) / gate_total
    probs_grad = jnp.sum(picked_grad[:, :, None] * chosen, axis=1)
    logit_grad = router_probs * (
        probs_grad - jnp.sum(probs_grad * router_probs, axis=-1, keepdims=True)
    )
    router_grad = jnp.dot(normed_float.T, logit_grad, precision=highest)
    normed_grad = jnp.dot(logit_grad, router.T, precision=highest) + from_slots(
        jnp.logical_or(place_first, place_second), rows_grad_back
    )
    scaled_two = normed_grad * gain_two
    hidden_grad = (
        upstream
        + scale_two * scaled_two
        - hidden_one * scale_two**3 * jnp.mean(scaled_two * hidden_one, axis=-1, keepdims=True)
    )
    gain_two_grad = jnp.sum(normed_grad * hidden_one * scale_two, axis=0)
    branch_grad = hidden_grad.astype(low)
    context_grad = lax.dot_general(
        branch_grad, full_out, (((1,), (1,)), ((), ())), preferred_element_type=full
    ).astype(low)
    context_grad_pieces = jnp.transpose(context_grad.reshape(rows, exps, head_cols), (1, 0, 2))
    context_grad_mine = swap(context_grad_pieces, "exp").reshape(exps, rows, heads, head_dim)
    branch_group = spread(branch_grad, "exp").reshape(exps * rows, width)
    out_grad = transposed_dot(context_mine.reshape(exps * rows, head_cols), branch_group).astype(low)

    scores = scores_of()
    probs_again = jnp.exp(scores - log_total)
    weights_again = probs_again.astype(low)
    values_grad = jnp.einsum(
        "shij,sihd->sjhd", weights_again, context_grad_mine, preferred_element_type=full
    )
    probs_grad_att = jnp.einsum(
        "sihd,sjhd->shij", context_grad_mine, values, preferred_element_type=full
    )
    row_delta = jnp.sum(probs_grad_att * probs_again, axis=-1, keepdims=True)
    scores_grad = (probs_again * (probs_grad_att - row_delta)).astype(low)
    scores_grad_sum = jnp.sum(scores_grad.astype(full), axis=0)
    bias_grad_mine = jnp.einsum("hij,ijb->bh", scores_grad_sum, onehot, precision=highest)
    bias_grad = lax.dynamic_update_slice_in_dim(
        jnp.zeros((BUCKETS, HEADS), full), bias_grad_mine, place * heads, 1
    )
    queries_grad = (
        jnp.einsum("shij,sjhd->sihd", scores_grad, key_rows, preferred_element_type=full)
        * score_scale
    )
    keys_grad = (
        jnp.einsum("shij,sihd->sjhd", scores_grad, queries, preferred_element_type=full)
        * score_scale
    )
    qkv_grad = (
        jnp.stack([queries_grad, keys_grad, values_grad], axis=2)
        .astype(low)
        .reshape(exps * rows, 3 * head_cols)
    )
    normed_one_part = lax.dot_general(
        qkv_grad, qkv_mine, (((1,), (1,)), ((), ())), preferred_element_type=full
    ).astype(low)
    normed_one_grad = jnp.sum(
        swap(normed_one_part.reshape(exps, rows, width), "exp").astype(full), axis=0
    )
    scaled_one = normed_one_grad * gain_one
    token_grad = (
        hidden_grad
        + scale_one * scaled_one
        - x_float * scale_one**3 * jnp.mean(scaled_one * x_float, axis=-1, keepdims=True)
    )
    gain_one_grad = jnp.sum(normed_one_grad * x_float * scale_one, axis=0)

    qkv_weight_grad = transposed_dot(normed_group, qkv_grad).astype(low)
    qkv_grad_rows = swap(qkv_weight_grad.reshape(exps, row_block, 3 * head_cols), "exp")
    qkv_grad_rows = jnp.transpose(
        qkv_grad_rows.reshape(exps, row_block, 3, head_cols), (1, 2, 0, 3)
    ).reshape(row_block, reps, -1)
    qkv_share = jnp.sum(
        swap(jnp.transpose(qkv_grad_rows, (1, 0, 2)), REP).astype(full), axis=0
    )
    out_pieces = jnp.transpose(out_grad.reshape(row_block, reps, -1), (1, 0, 2))
    out_share = jnp.sum(swap(out_pieces, REP).astype(full), axis=0)

    small = jnp.concatenate(
        [
            router_grad.reshape(-1),
            jnp.stack([gain_one_grad, gain_two_grad], axis=1).reshape(-1),
            bias_grad.reshape(-1),
        ]
    ).reshape(-1, 128)
    small_total = jnp.sum(lax.all_gather(small, ALL, axis=0, tiled=False), axis=0).reshape(-1)
    router_total = small_total[: router.size].reshape(router.shape)
    gains_total = small_total[router.size : router.size + norm_gains.size].reshape(norm_gains.shape)
    bias_total = small_total[router.size + norm_gains.size :].reshape(rel_bias.shape)

    qkv_new = adamw_update(attn_qkv, qkv_first, qkv_second, qkv_share, 1.5 / math.sqrt(D), 0.1)
    out_new = adamw_update(attn_out, out_first, out_second, out_share, 6.0 / math.sqrt(D), 0.1)
    bias_new = adamw_update(rel_bias, bias_first, bias_second, bias_total, 0.3, 0.0)
    router_new = adamw_update(
        router, router_first, router_second, router_total, 1.0 / math.sqrt(D), 0.1
    )
    gains_new = adamw_update(norm_gains, gains_first, gains_second, gains_total, 0.5, 0.0)
    in_new = adamw_update(expert_in, in_first, in_second, in_share, 1.5 / math.sqrt(D), 0.1)
    down_new = adamw_update(
        expert_out, down_first, down_second, down_share, 1.5 / math.sqrt(FF), 0.1
    )
    return (
        (block_out, token_grad)
        + qkv_new
        + out_new
        + bias_new
        + router_new
        + gains_new
        + in_new
        + down_new
    )


def solution(mesh):
    reps, exps = mesh.devices.shape
    split = Mesh(mesh.devices.reshape(reps // QUAD, QUAD, exps), ALL)
    by_rows = P(ALL, None)
    attn = P("exp", REP)
    expert = P("exp", REP, None)
    return jax.shard_map(
        per_device if (reps, exps) == (2 * QUAD, 4) else plain_device,
        mesh=split,
        in_specs=(by_rows, by_rows) + (P(),) * 3 + (attn,) * 6 + (P(),) * 9 + (expert,) * 6,
        out_specs=(by_rows, by_rows) + (attn,) * 6 + (P(),) * 9 + (expert,) * 6,
        check_vma=False,
    )
```

```python
import functools
import math

import jax
import jax.numpy as jnp
from jax import lax
from jax.experimental import pallas as pl
from jax.experimental.pallas import tpu as pltpu
from jax.sharding import Mesh
from jax.sharding import PartitionSpec as P

D = 1024
HEADS = 16
FF = 2816
BUCKETS = 32
STEP = 10
QUAD = 4
REP = ("grp", "quad")
PLANE = ("quad", "exp")
ALL = ("grp", "quad", "exp")

highest = lax.Precision.HIGHEST
eps_norm = 1e-06
thresholds = (1, 2, 3, 4, 5, 6, 7, 8, 11, 16, 22, 32, 45, 64, 90)
beta_one = 0.9
beta_two = 0.999
eps_adam = 1e-08
low = jnp.bfloat16
full = jnp.float32
MESH = pl.DeviceIdType.MESH


def adamw_update(weight, moment, second, gradient, step_rate, decay_factor):
    new_moment = beta_one * moment + (1.0 - beta_one) * gradient
    new_second = beta_two * second + (1.0 - beta_two) * gradient * gradient
    corrected = new_moment / (1.0 - beta_one**STEP)
    scaled = new_second / (1.0 - beta_two**STEP)
    new_weight = weight - step_rate * (
        corrected / (jnp.sqrt(scaled) + eps_adam) + decay_factor * weight
    )
    return (new_moment, new_second, new_weight)


def gated_unit(gate_input, up_input):
    return jax.nn.gelu(gate_input, approximate=True) * up_input


def dot(a, b):
    return jnp.dot(a, b, preferred_element_type=full)


def nt(a, b, precision=None):
    return lax.dot_general(a, b, (((1,), (1,)), ((), ())), preferred_element_type=full, precision=precision)


def tn(a, b):
    return lax.dot_general(a, b, (((0,), (0,)), ((), ())), preferred_element_type=full)


class Where:
    def __init__(self, grps, exps):
        self.grps, self.exps = grps, exps
        self.reps = grps * QUAD
        self.grp = lax.axis_index("grp")
        self.quad = lax.axis_index("quad")
        self.exp = lax.axis_index("exp")
        self.rep = self.grp * QUAD + self.quad
        self.base = self.rep * exps
        self.me = self.base + self.exp

    def device(self, rep, exp):
        return (rep // QUAD, rep % QUAD, exp)

    def near(self, flip):
        q = self.quad
        if flip & 1:
            q = q + 1 - 2 * (q % 2)
        if flip & 2:
            q = q + 2 - 4 * (q // 2)
        return q


def send(src, dst, send_sem, recv_sem, device):
    return pltpu.make_async_remote_copy(
        src_ref=src, dst_ref=dst, send_sem=send_sem, recv_sem=recv_sem, device_id=device, device_id_type=MESH
    )


def arrived(ref, sem):
    pltpu.make_async_copy(ref, ref, sem).wait()


def greet_all(at):
    count = at.reps * at.exps
    barrier = pltpu.get_barrier_semaphore()

    def greet(k, _):
        other = (at.me + k) % count
        pl.semaphore_signal(
            barrier, inc=1, device_id=at.device(other // at.exps, other % at.exps), device_id_type=MESH
        )
        return 0

    lax.fori_loop(1, count, greet, 0)
    pl.semaphore_wait(barrier, count - 1)


def lane_of(shape):
    return lax.broadcasted_iota(jnp.int32, shape, 1)


def row_of(shape):
    return lax.broadcasted_iota(jnp.int32, shape, 0)


def bucket_of(offset):
    distance = jnp.abs(offset)
    bucket = jnp.where(offset > 0, 16, 0)
    for threshold in thresholds:
        bucket = bucket + jnp.where(distance >= threshold, 1, 0)
    return bucket


def bits_of(count):
    return count.bit_length() - 1


def column_parts(width):
    tiles = width // 128
    cuts = [0, (tiles + 2) // 3, (2 * tiles + 2) // 3, tiles]
    return [(cuts[i] * 128, (cuts[i + 1] - cuts[i]) * 128) for i in range(3)]


def flipped(place, bit):
    return place + (1 - 2 * ((place // (1 << bit)) % 2)) * (1 << bit)


class Doubling:
    def __init__(self, at, own, every, sems, core_sems, orders):
        self.at, self.own, self.every = at, own, every
        self.sems, self.core_sems, self.orders = sems, core_sems, orders
        self.plane = at.quad * at.exps + at.exp
        self.steps = len(orders[0])
        self.parts = column_parts(own.shape[1])

    def device(self, bit):
        other = flipped(self.plane, bit)
        return (self.at.grp, other // self.at.exps, other % self.at.exps)

    def place(self, part, j):
        p = self.plane
        for i, bit in enumerate(self.orders[part]):
            if (j >> i) & 1:
                p = flipped(p, bit + 1)
        return p

    def block(self, part, p):
        begin, size = self.parts[part]
        return self.every.at[p, :, pl.ds(begin, size)]

    def source(self, part, j):
        begin, size = self.parts[part]
        return self.own.at[:, pl.ds(begin, size)] if j == 0 else self.block(part, self.place(part, j))

    def index(self, step, part, j):
        return part * (1 << self.steps) + (1 << step) - 1 + j

    def copy(self, step, part, j):
        i = self.index(step, part, j)
        return send(
            self.source(part, j),
            self.block(part, self.place(part, j)),
            self.sems.at[0, i],
            self.sems.at[1, i],
            self.device(self.orders[part][step] + 1),
        )

    def core_copy(self, part, j):
        i = part * (1 << self.steps) + j
        return send(
            self.source(part, j),
            self.block(part, self.place(part, j)),
            self.core_sems.at[0, i],
            self.core_sems.at[1, i],
            self.device(0),
        )

    def start(self):
        for part in range(3):
            for step in range(self.steps):
                self.copy(step, part, 0).start()
        for part in range(3):
            self.core_copy(part, 0).start()
        self.keep().start()

    def keep(self):
        return pltpu.make_async_copy(self.own, self.every.at[self.plane], self.core_sems.at[1, 3 << self.steps])

    def next(self, step):
        for part in range(3):
            for j in range(1 << step):
                k = (1 << step) + j
                arrived(self.block(part, self.place(part, k)), self.sems.at[1, self.index(step, part, j)])
                for later in range(step + 1, self.steps):
                    self.copy(later, part, k).start()
                self.core_copy(part, k).start()

    def finish_in(self):
        for part in range(3):
            for j in range(1 << self.steps):
                there = self.block(part, flipped(self.place(part, j), 0))
                arrived(there, self.core_sems.at[1, part * (1 << self.steps) + j])
        self.keep().wait()

    def finish_out(self):
        for part in range(3):
            for j in range(1 << self.steps):
                self.core_copy(part, j).wait_send()
            for step in range(self.steps):
                for j in range(1 << step):
                    self.copy(step, part, j).wait_send()


class Tiles:
    def __init__(self, units, reps):
        self.units = units
        self.reps = reps
        self.hidden = units * reps
        self.half = self.hidden // 256
        self.wide = (self.half + 1) // 2
        self.count = 3
        self.size = 128 * self.wide // self.count
        self.skip = 128 * (2 * self.wide - self.half)

    def start(self, quad):
        return 128 * (self.half * (quad // 2) + (self.half - self.wide) * (quad % 2))

    def rows(self, tile):
        result = []
        for k in range(QUAD):
            found = None
            for parity in range(2):
                first = self.start(parity) + tile * self.size
                live = first + (self.skip if parity and tile == 0 else 0)
                begin = max(live, k * self.units)
                end = min(first + self.size, (k + 1) * self.units)
                if end > begin:
                    found = (begin - k * self.units, end - begin, parity, begin - first)
            result.append(found)
        return result


class Outward:
    def __init__(self, at, tiles, tile, in_low, down_slab, both_w, down_w, nothing, sems, down_sems):
        self.at, self.tiles, self.tile = at, tiles, tile
        self.in_low, self.down_slab, self.both_w, self.down_w = in_low, down_slab, both_w, down_w
        self.nothing, self.sems, self.down_sems = nothing, sems, down_sems
        self.slab = in_low.shape[0]

    def source(self, quad, section):
        begin = section * self.tiles.hidden + self.tiles.start(quad) + self.tile * self.tiles.size
        return self.in_low.at[:, pl.ds(pl.multiple_of(begin, 128), self.tiles.size)]

    def target(self, rep, section):
        rows = pl.ds(pl.multiple_of(rep * self.slab, self.slab), self.slab)
        return self.both_w.at[rows, pl.ds(section * self.tiles.size, self.tiles.size)]

    def over(self, act):
        at = self.at

        def one(k, _):
            other = (at.rep + k) % at.reps
            for section in range(2):
                act(
                    functools.partial(
                        send,
                        self.source(other % QUAD, section),
                        self.target(at.rep, section),
                        self.sems.at[0, section * at.reps + other],
                        self.sems.at[1, section * at.reps + at.rep],
                        at.device(other, at.exp),
                    )
                )
            return 0

        lax.fori_loop(1, at.reps, one, 0)

    def over_down(self, act, act_local):
        at = self.at
        for k, piece in enumerate(self.tiles.rows(self.tile)):
            if piece is None:
                continue
            begin, count, parity, to = piece
            quad = 2 * (at.rep // QUAD) + parity
            src, dst = self.down_slab.at[pl.ds(begin, count)], self.down_w.at[pl.ds(to, count)]
            recv = self.down_sems.at[1, at.rep]
            for g in range(at.grps):
                stays = jnp.logical_and(at.grp == g, at.quad == quad)
                ours = at.rep % QUAD == k

                @pl.when(jnp.logical_and(ours, jnp.logical_not(stays)))
                def _():
                    act(functools.partial(send, src, dst, self.down_sems.at[0, g], recv, (g, quad, at.exp)))

                @pl.when(jnp.logical_and(ours, stays))
                def _():
                    act_local(functools.partial(pltpu.make_async_copy, src, dst, recv))

    def blank(self):
        return pltpu.make_async_copy(
            self.nothing, self.down_w.at[pl.ds(0, self.tiles.skip)], self.down_sems.at[1, self.at.reps]
        )

    def start(self):
        at = self.at
        self.over_down(lambda copy: copy().start(), lambda copy: copy().start())
        self.over(lambda copy: copy().start())
        for section in range(2):
            pltpu.make_async_copy(
                self.source(at.quad, section), self.target(at.rep, section), self.sems.at[1, section * at.reps + at.rep]
            ).start()
        if self.tile == 0:

            @pl.when(at.quad % 2 == 1)
            def _():
                self.blank().start()

    def arrive(self):
        at = self.at

        def one(rep, _):
            for section in range(2):
                arrived(self.target(rep, section), self.sems.at[1, section * at.reps + rep])
            return 0

        lax.fori_loop(0, at.reps, one, 0)
        for parity in range(2):

            @pl.when(at.quad % 2 == parity)
            def _():
                for k, piece in enumerate(self.tiles.rows(self.tile)):
                    if piece is not None and piece[2] == parity:
                        source = QUAD * (at.quad // 2) + k
                        arrived(self.down_w.at[pl.ds(piece[3], piece[1])], self.down_sems.at[1, source])
                if parity and self.tile == 0:
                    self.blank().wait()

    def sent(self):
        self.over(lambda copy: copy().wait_send())
        self.over_down(lambda copy: copy().wait_send(), lambda copy: None)


class Homeward:
    def __init__(self, at, tiles, tile, both, down, in_parts, down_parts, sems, down_sems):
        self.at, self.tiles, self.tile = at, tiles, tile
        self.both, self.down, self.in_parts, self.down_parts = both, down, in_parts, down_parts
        self.sems, self.down_sems = sems, down_sems
        self.slab = in_parts.shape[1]

    def target(self, grp, quad, parity, section):
        skip = self.tiles.skip if parity and self.tile == 0 else 0
        to = section * self.tiles.hidden + self.tiles.start(quad) + self.tile * self.tiles.size + skip
        to = to if isinstance(to, int) else pl.multiple_of(to, 128)
        return skip, self.in_parts.at[grp, :, pl.ds(to, self.tiles.size - skip)]

    def copy(self, rep, parity, section, local=False):
        at = self.at
        skip, dst = self.target(at.grp, at.quad, parity, section)
        rows = pl.ds(pl.multiple_of(rep * self.slab, self.slab), self.slab)
        src = self.both.at[rows, pl.ds(section * self.tiles.size + skip, self.tiles.size - skip)]
        recv = self.sems.at[1, section * at.reps + at.rep]
        if local:
            return pltpu.make_async_copy(src, dst, recv)
        return send(src, dst, self.sems.at[0, section * at.reps + rep], recv, at.device(rep, at.exp))

    def over(self, act, act_local):
        at = self.at
        for parity in range(2):

            @pl.when(at.quad % 2 == parity)
            def _():
                def one(k, _):
                    for section in range(2):
                        act(self.copy((at.rep + k) % at.reps, parity, section))
                    return 0

                lax.fori_loop(1, at.reps, one, 0)
                if act_local:
                    for section in range(2):
                        act_local(self.copy(at.rep, parity, section, local=True))

    def over_down(self, act, act_local):
        at = self.at
        for k, piece in enumerate(self.tiles.rows(self.tile)):
            if piece is None:
                continue
            begin, count, parity, to = piece
            src, dst = self.down.at[pl.ds(to, count)], self.down_parts.at[at.grp, pl.ds(begin, count)]
            recv = self.down_sems.at[1, at.grp]
            stays = jnp.logical_and(at.grp == at.quad // 2, at.quad == k)
            ours = at.quad % 2 == parity

            @pl.when(jnp.logical_and(ours, jnp.logical_not(stays)))
            def _():
                act(functools.partial(send, src, dst, self.down_sems.at[0, k], recv, (at.quad // 2, k, at.exp)))

            @pl.when(jnp.logical_and(ours, stays))
            def _():
                act_local(functools.partial(pltpu.make_async_copy, src, dst, recv))

    def start(self):
        self.over_down(lambda copy: copy().start(), lambda copy: copy().start())
        self.over(lambda copy: copy.start(), lambda copy: copy.start())

    def arrive(self):
        at = self.at
        for rep in range(at.reps):
            for section in range(2):
                _, dst = self.target(rep // QUAD, rep % QUAD, rep % 2, section)
                arrived(dst, self.sems.at[1, section * at.reps + rep])
        for k, piece in enumerate(self.tiles.rows(self.tile)):
            if piece is None:
                continue

            @pl.when(at.quad == k)
            def _():
                for g in range(at.grps):
                    arrived(self.down_parts.at[g, pl.ds(piece[0], piece[1])], self.down_sems.at[1, g])

    def sent(self):
        self.over(lambda copy: copy.wait_send(), None)
        self.over_down(lambda copy: copy().wait_send(), lambda copy: None)


def forward_kernel(
    grps,
    exps,
    lengths,
    rel_bias,
    routes_col,
    tokens,
    cotangent,
    gains,
    router,
    qkv_t,
    out_w,
    in_low,
    down_slab,
    both_w,
    down_w,
    cot_all,
    n_all,
    comb_all,
    qkv_out,
    lse_out,
    mine_out,
    n1_out,
    wqkv_out,
    wout_out,
    h1_out,
    n2_out,
    probs_out,
    tok_all,
    wqkv,
    wout,
    n1,
    qkv,
    lse,
    mine,
    ctx,
    bias,
    comb_send,
    nothing,
    tok_sem,
    wq_sem,
    wo_sem,
    wo2_sem,
    weight_sem,
    down_sem,
    ctx_sem,
    cot_sem,
    cot_core_sem,
    n_sem,
    n_core_sem,
    comb_sem,
    store_sem,
):
    at = Where(grps, exps)
    reps = at.reps
    rows, width = tokens.shape
    heads = HEADS // exps
    head_dim = width // HEADS
    head_cols = heads * head_dim
    block_cols = min(128, head_cols)
    shard_cols, row_block = qkv_t.shape
    seg = math.gcd(shard_cols, head_cols)
    segs = shard_cols // seg
    tiles = Tiles(down_slab.shape[0], reps)
    plane = at.quad * exps + at.exp
    members = QUAD * exps
    scale = 1.0 / math.sqrt(head_dim)
    SEND, RECV = 0, 1

    greet_all(at)

    def exp_peer(k):
        return (at.exp + k) % exps

    for k in range(1, exps):
        peer = exp_peer(k)
        send(
            tokens, tok_all.at[at.exp], tok_sem.at[SEND, peer], tok_sem.at[RECV, at.exp], at.device(at.rep, peer)
        ).start()
    tok_all[at.exp] = tokens[...]

    def segment(k):
        col = (at.rep * segs + k) * seg
        section = col // width
        within = col - section * width
        owner = within // head_cols
        return owner, section * head_cols + within - owner * head_cols

    def segment_copy(k, shift):
        owner, offset = segment(k)
        src = qkv_t.at[pl.ds(k * seg, seg)]
        dst = wqkv.at[at.exp, pl.ds(pl.multiple_of(offset, seg), seg)]
        target = at.device((at.rep + shift) % reps, owner)
        return owner, src, dst, send(
            src, dst, wq_sem.at[SEND, k * reps + shift], wq_sem.at[RECV, at.exp * 3 * (head_cols // seg) + offset // seg], target
        )

    def over_segments(act, act_local):
        def one(i, _):
            k, shift = i // reps, i % reps
            owner, src, dst, copy = segment_copy(k, shift)
            stays = jnp.logical_and(shift == 0, owner == at.exp)

            @pl.when(jnp.logical_not(stays))
            def _():
                act(copy)

            @pl.when(stays)
            def _():
                act_local(k, src, dst)

            return 0

        lax.fori_loop(0, segs * reps, one, 0)

    def local_segment(k, src, dst):
        _, offset = segment(k)
        pltpu.make_async_copy(src, dst, wq_sem.at[RECV, at.exp * 3 * (head_cols // seg) + offset // seg]).start()

    over_segments(lambda copy: copy.start(), local_segment)

    for k in range(1, reps):
        other = (at.rep + k) % reps
        send(
            out_w, wout.at[at.exp, at.rep], wo_sem.at[SEND, other], wo_sem.at[RECV, at.rep], at.device(other, at.exp)
        ).start()
    wout[at.exp, at.rep] = out_w[...]
    chip_bits = list(range(bits_of(members) - 1))
    cots = Doubling(at, cotangent, cot_all, cot_sem, cot_core_sem, [chip_bits[::-1]] * 3)
    cots.start()

    span = 2 * rows
    bucket = bucket_of(lane_of((8, span)) - rows)
    for h in range(heads):
        line = jnp.zeros((8, span), full)
        for b in range(BUCKETS):
            line = jnp.where(bucket == b, rel_bias[b, at.exp * heads + h], line)
        whole = jnp.broadcast_to(line[0:1], (rows, span))
        bias[h] = pltpu.roll(whole, 0, 1, stride=1, stride_axis=0)[:, rows:]

    def norm_group(s, _):
        @pl.when(s != at.exp)
        def _():
            arrived(tok_all.at[s], tok_sem.at[RECV, s])

        x = tok_all[s].astype(full)
        r = lax.rsqrt(jnp.mean(x * x, axis=1, keepdims=True) + eps_norm)
        n1[s] = (x * r * gains[0:1, :]).astype(low)
        return 0

    lax.fori_loop(0, exps, norm_group, 0)

    nothing[...] = jnp.zeros_like(nothing)
    weights = [
        Outward(
            at, tiles, t, in_low, down_slab, both_w.at[t], down_w.at[t], nothing, weight_sem.at[t], down_sem.at[t]
        )
        for t in range(2)
    ]
    weights[0].start()

    def wait_segment(i, _):
        e, j = i // (3 * head_cols // seg), i % (3 * head_cols // seg)
        arrived(wqkv.at[e, pl.ds(pl.multiple_of(j * seg, seg), seg)], wq_sem.at[RECV, i])
        return 0

    lax.fori_loop(0, exps * 3 * head_cols // seg, wait_segment, 0)

    def project(s, _):
        total = jnp.zeros((rows, 3 * head_cols), full)
        for e in range(exps):
            total = total + nt(n1[s, :, e * row_block : (e + 1) * row_block], wqkv[e])
        qkv[s] = total.astype(low)
        return 0

    lax.fori_loop(0, exps, project, 0)

    for k in range(1, reps):
        other = (at.rep + k) % reps
        arrived(wout.at[at.exp, other], wo_sem.at[RECV, other])

    def wout_copies():
        return [
            send(
                wout.at[at.exp],
                wout.at[at.exp],
                wo2_sem.at[SEND, exp_peer(k)],
                wo2_sem.at[RECV, at.exp],
                at.device(at.rep, exp_peer(k)),
            )
            for k in range(1, exps)
        ]

    for copy in wout_copies():
        copy.start()

    cots.next(0)

    def attend(i, _):
        s = (at.exp + 1 + i) % exps
        ok = lane_of((rows, rows)) < lengths[at.base + s]
        lane = lane_of((rows, block_cols))
        sums = jnp.zeros((rows, 128), full)
        for c in range(head_cols // block_cols):
            cols = slice(c * block_cols, (c + 1) * block_cols)
            q = qkv[s, :, cols]
            k = qkv[s, :, head_cols + c * block_cols : head_cols + (c + 1) * block_cols]
            v = qkv[s, :, 2 * head_cols + c * block_cols : 2 * head_cols + (c + 1) * block_cols]
            result = jnp.zeros((rows, block_cols), full)
            for t in range(block_cols // head_dim):
                h = c * (block_cols // head_dim) + t
                here = jnp.logical_and(lane >= t * head_dim, lane < (t + 1) * head_dim)
                scores = nt(jnp.where(here, q, jnp.zeros_like(q)), k) * scale + bias[h]
                scores = jnp.where(ok, scores, -1e30)
                top = jnp.max(scores, axis=1, keepdims=True)
                weights = jnp.exp(scores - top)
                total = jnp.sum(weights, axis=1, keepdims=True)
                weights = (weights * (1.0 / total)).astype(low)
                result = jnp.where(here, jnp.dot(weights, v, preferred_element_type=full), result)
                sums = jnp.where(lane_of((rows, 128)) == h, top + jnp.log(total), sums)
            mine[s, :, cols] = result.astype(low)
        lse[s] = sums

        @pl.when(i < exps - 1)
        def _():
            send(
                mine.at[s], ctx.at[at.exp], ctx_sem.at[SEND, s], ctx_sem.at[RECV, at.exp], at.device(at.rep, s)
            ).start()

        @pl.when(i == exps - 1)
        def _():
            pltpu.make_async_copy(mine.at[s], ctx.at[at.exp], ctx_sem.at[RECV, at.exp]).start()

        return 0

    lax.fori_loop(0, exps, attend, 0)

    cots.next(1)
    for k in range(1, exps):
        arrived(wout.at[exp_peer(k)], wo2_sem.at[RECV, exp_peer(k)])
    for e in range(exps):
        arrived(ctx.at[e], ctx_sem.at[RECV, e])

    out_cols = wout.shape[3]
    for r in range(reps):
        cols = slice(r * out_cols, (r + 1) * out_cols)
        total = tokens[:, cols].astype(full)
        for e in range(exps):
            total = total + jnp.dot(ctx[e], wout[e, r], preferred_element_type=full)
        h1_out[:, cols] = total
    h1 = h1_out[...]
    r2 = lax.rsqrt(jnp.mean(h1 * h1, axis=1, keepdims=True) + eps_norm)
    n2 = (h1 * r2 * gains[1:2, :]).astype(low)
    n2_out[...] = n2
    rotated = [chip_bits[c:] + chip_bits[:c] for c in range(3)]
    rows_two = Doubling(at, n2_out, n_all, n_sem, n_core_sem, rotated)
    rows_two.start()
    weights[1].start()

    logits = jnp.dot(n2.astype(full), router[...], precision=highest, preferred_element_type=full)
    lane = lane_of((rows, 128))
    logits = jnp.where(lane < exps, logits, -1e30)
    probs = jnp.exp(logits - jnp.max(logits, axis=1, keepdims=True))
    probs = probs / jnp.sum(probs, axis=1, keepdims=True)
    probs_out[...] = probs
    mine_hot = jnp.logical_or(lane == routes_col[:, 0:1], lane == routes_col[:, 1:2])
    picked = jnp.where(mine_hot, probs, 0.0)
    comb = picked / jnp.sum(picked, axis=1, keepdims=True)
    comb = jnp.where(row_of((rows, 1)) < lengths[at.me], comb, 0.0)
    comb_send[...] = comb.T[0 : comb_send.shape[0]]

    def comb_copy(k):
        other = (plane + k) % members
        return send(
            comb_send,
            comb_all.at[plane],
            comb_sem.at[SEND, other],
            comb_sem.at[RECV, plane],
            (at.grp, other // exps, other % exps),
        )

    def start_comb(k, _):
        comb_copy(k).start()
        return 0

    lax.fori_loop(1, members, start_comb, 0)
    pltpu.make_async_copy(comb_send, comb_all.at[plane], comb_sem.at[RECV, plane]).start()
    rows_two.next(0)

    stores = [
        (qkv, qkv_out),
        (lse, lse_out),
        (mine, mine_out),
        (n1, n1_out),
        (wqkv, wqkv_out),
        (wout, wout_out),
    ]
    for i, (src, dst) in enumerate(stores):
        pltpu.make_async_copy(src, dst, store_sem.at[i]).start()

    for step in range(1, rows_two.steps):
        rows_two.next(step)
    for step in range(2, cots.steps):
        cots.next(step)

    cots.finish_in()
    rows_two.finish_in()

    def comb_in(k, _):
        arrived(comb_all.at[k], comb_sem.at[RECV, k])
        return 0

    lax.fori_loop(0, members, comb_in, 0)
    for tile in weights:
        tile.arrive()

    for k in range(1, exps):
        peer = exp_peer(k)
        arrived(tokens, tok_sem.at[SEND, peer])
        arrived(mine.at[peer], ctx_sem.at[SEND, peer])
    over_segments(lambda copy: copy.wait_send(), lambda k, src, dst: None)
    for k in range(1, reps):
        arrived(out_w, wo_sem.at[SEND, (at.rep + k) % reps])
    for copy in wout_copies():
        copy.wait_send()
    cots.finish_out()
    rows_two.finish_out()

    def sent_comb(k, _):
        comb_copy(k).wait_send()
        return 0

    lax.fori_loop(1, members, sent_comb, 0)
    for tile in weights:
        tile.sent()
    for i, (src, dst) in enumerate(stores):
        pltpu.make_async_copy(src, dst, store_sem.at[i]).wait()


def forward_call(
    grps, exps, lengths, rel_bias, routes_col, tokens, cotangent, gains, router, qkv_t, out_w, in_low, down_slab
):
    reps = grps * QUAD
    rows, width = tokens.shape
    head_cols = width // exps
    row_block = qkv_t.shape[1]
    seg = math.gcd(qkv_t.shape[0], head_cols)
    segs = qkv_t.shape[0] // seg
    units = down_slab.shape[0]
    out_cols = out_w.shape[1]
    heads = HEADS // exps
    members = QUAD * exps
    tiles = Tiles(units, reps)
    shape = jax.ShapeDtypeStruct
    vmem = pl.BlockSpec(memory_space=pltpu.VMEM)
    smem = pl.BlockSpec(memory_space=pltpu.SMEM)
    hbm = pl.BlockSpec(memory_space=pl.ANY)
    results = [
        (shape((2, width, 2 * tiles.size), low), hbm),
        (shape((2, tiles.size, width), low), hbm),
        (shape((members, rows, width), low), hbm),
        (shape((members, rows, width), low), hbm),
        (shape((members, 8, rows), full), hbm),
        (shape((exps, rows, 3 * head_cols), low), hbm),
        (shape((exps, rows, 128), full), hbm),
        (shape((exps, rows, head_cols), low), hbm),
        (shape((exps, rows, width), low), hbm),
        (shape((exps, 3 * head_cols, row_block), low), hbm),
        (shape((exps, reps, row_block, out_cols), low), hbm),
        (shape((rows, width), full), vmem),
        (shape((rows, width), low), vmem),
        (shape((rows, 128), full), vmem),
    ]
    dma = pltpu.SemaphoreType.DMA
    chips = members // 2
    return pl.pallas_call(
        functools.partial(forward_kernel, grps, exps),
        out_shape=[r[0] for r in results],
        in_specs=[smem] * 2 + [vmem] * 7 + [hbm] * 2,
        out_specs=[r[1] for r in results],
        scratch_shapes=[
            pltpu.VMEM((exps, rows, width), low),
            pltpu.VMEM((exps, 3 * head_cols, row_block), low),
            pltpu.VMEM((exps, reps, row_block, out_cols), low),
            pltpu.VMEM((exps, rows, width), low),
            pltpu.VMEM((exps, rows, 3 * head_cols), low),
            pltpu.VMEM((exps, rows, 128), full),
            pltpu.VMEM((exps, rows, head_cols), low),
            pltpu.VMEM((exps, rows, head_cols), low),
            pltpu.VMEM((heads, rows, rows), full),
            pltpu.VMEM((8, rows), full),
            pltpu.VMEM((tiles.skip, width), low),
            dma((2, exps)),
            dma((2, max(segs * reps, exps * 3 * head_cols // seg))),
            dma((2, reps)),
            dma((2, exps)),
            dma((2, 2, 2 * reps)),
            dma((2, 2, reps + 1)),
            dma((2, exps)),
            dma((2, 3 * chips)),
            dma((2, 3 * chips + 1)),
            dma((2, 3 * chips)),
            dma((2, 3 * chips + 1)),
            dma((2, members)),
            dma((6,)),
        ],
        compiler_params=pltpu.CompilerParams(
            collective_id=0, has_side_effects=True, vmem_limit_bytes=60 * 1024 * 1024
        ),
        name="forward",
    )(lengths, rel_bias, routes_col, tokens, cotangent, gains, router, qkv_t, out_w, in_low, down_slab)


def expert_kernel(
    grps,
    exps,
    cap,
    order,
    routes,
    comb,
    n_all,
    cot_all,
    both_w,
    down_w,
    in_low,
    down_slab,
    n_sum,
    y_sum,
    c_sum,
    both_g,
    down_g,
    in_parts,
    down_parts,
    place,
    marks,
    n_rows,
    g_rows,
    both_v,
    down_v,
    raw_n,
    raw_g,
    y_acc,
    n_acc,
    both_d,
    active,
    both_stage,
    down_stage,
    out_n,
    out_y,
    load_sem,
    raw_sem,
    out_sem,
    in_sem,
    in_down_sem,
    home_sem,
    home_down_sem,
    stage_sem,
):
    at = Where(grps, exps)
    rows, width = n_all.shape[1:]
    tiles = Tiles(down_slab.shape[0], at.reps)
    size = tiles.size
    slots = exps * cap
    loads = [pltpu.make_async_copy(both_w.at[t], both_v.at[t], load_sem.at[0, t]) for t in range(2)] + [
        pltpu.make_async_copy(down_w.at[t], down_v.at[t], load_sem.at[1, t]) for t in range(2)
    ]
    for copy in loads:
        copy.start()

    def raw_copies(q):
        here = pl.ds(pl.multiple_of(q * exps, exps), exps)
        return [
            pltpu.make_async_copy(n_all.at[here], raw_n.at[q % 2], raw_sem.at[0, q % 2]),
            pltpu.make_async_copy(cot_all.at[here], raw_g.at[q % 2], raw_sem.at[1, q % 2]),
        ]

    for copy in raw_copies(0):
        copy.start()
    greet_all(at)
    last = tiles.count - 1
    incoming = Outward(
        at, tiles, last, in_low, down_slab, both_v.at[last], down_v.at[last], None, in_sem, in_down_sem
    )
    incoming.start()
    home = Homeward(
        at, tiles, 0, both_stage.at[0], down_stage.at[0], in_parts, down_parts, home_sem, home_down_sem
    )

    earlier = jnp.where(row_of((rows, rows)) < lane_of((rows, rows)), 1.0, 0.0).astype(low)
    slot = row_of((cap, rows)).astype(full)

    def dispatch(q, _):
        @pl.when(q + 1 < QUAD)
        def _():
            for copy in raw_copies(q + 1):
                copy.start()

        for copy in raw_copies(q):
            copy.wait()
        hot = jnp.logical_or(routes[q, 0] == at.exp, routes[q, 1] == at.exp)
        hot_low = jnp.where(hot, 1.0, 0.0).astype(low)
        before = dot(hot_low, earlier)
        for j in range(exps):
            s = q * exps + j
            inside = jnp.logical_and(slot == before[j : j + 1, :], hot_low[j : j + 1, :].astype(full) > 0.5)
            here = jnp.where(inside, 1.0, 0.0)
            place[s] = here.astype(low)
            g = raw_g[q % 2, 0]
            for b in range(1, exps):
                g = jnp.where(order[s] == q * exps + b, raw_g[q % 2, b], g)
            where = pl.ds(pl.multiple_of(s * cap, cap), cap)
            n_rows[where] = dot(here.astype(low), raw_n[q % 2, j]).astype(low)
            g_rows[where] = dot(here.astype(low), g).astype(low)
            marks[where, 0:1] = jnp.sum(here * comb[s, pl.ds(at.exp, 1), :], axis=1, keepdims=True)
            marks[where, 1:2] = jnp.zeros((cap, 1), full)
        return 0

    lax.fori_loop(0, QUAD, dispatch, 0)
    for copy in loads:
        copy.wait()
    curve = math.sqrt(2.0 / math.pi)

    def tile_work(f, _):
        @pl.when(f == last)
        def _():
            incoming.arrive()

        def chunk(c, _):
            here = pl.ds(pl.multiple_of(c * slots, slots), slots)
            share = marks[here, 0:1]
            both = dot(n_rows[here], both_v[f])
            gate_part, up_part = both[:, :size], both[:, size:]
            grad = nt(g_rows[here], down_v[f])
            square = gate_part * gate_part
            bend = jnp.tanh(curve * gate_part * (1.0 + 0.044715 * square))
            half = 0.5 * (1.0 + bend)
            gelu = gate_part * half
            slope = half + (0.5 * curve) * gate_part * (1.0 - bend * bend) * (1.0 + (3 * 0.044715) * square)
            value = gelu * up_part
            marks[here, 1:2] += jnp.sum(value * grad, axis=1, keepdims=True)
            grad = grad * share
            active[here] = (value * share).astype(low)
            both_d[here, :size] = (grad * up_part * slope).astype(low)
            both_d[here, size:] = (grad * gelu).astype(low)
            y = dot(active[here], down_v[f])
            y_acc[here] = jnp.where(f == 0, y, y_acc[here].astype(full) + y).astype(low)
            n_back = nt(both_d[here], both_v[f])
            n_acc[here] = jnp.where(f == 0, n_back, n_acc[here] + n_back)
            return 0

        lax.fori_loop(0, QUAD, chunk, 0)

        def columns(m, _):
            cols = pl.ds(pl.multiple_of(m * (width // 2), width // 2), width // 2)
            both_stage[f, cols] = tn(n_rows[:, cols], both_d[...]).astype(low)
            down_stage[f, :, cols] = tn(active[...], g_rows[:, cols]).astype(low)
            return 0

        lax.fori_loop(0, 2, columns, 0)

        @pl.when(f == 0)
        def _():
            home.start()

        @pl.when(f > 0)
        def _():
            for copy in stage_copies(f):
                copy.start()

        return 0

    def stage_copies(f):
        return [
            pltpu.make_async_copy(both_stage.at[f], both_g.at[f - 1], stage_sem.at[0, f]),
            pltpu.make_async_copy(down_stage.at[f], down_g.at[f - 1], stage_sem.at[1, f]),
        ]

    lax.fori_loop(0, tiles.count, tile_work, 0)

    def out_copies(s):
        return [
            pltpu.make_async_copy(out_n.at[s % 2], n_sum.at[s], out_sem.at[0, s % 2]),
            pltpu.make_async_copy(out_y.at[s % 2], y_sum.at[s], out_sem.at[1, s % 2]),
        ]

    members = QUAD * exps

    def gather(s, _):
        @pl.when(s >= 2)
        def _():
            for copy in out_copies(s - 2):
                copy.wait()

        where = pl.ds(pl.multiple_of(s * cap, cap), cap)
        out_n[s % 2] = tn(place[s], n_acc[where].astype(low)).astype(low)
        out_y[s % 2] = tn(place[s], y_acc[where]).astype(low)
        line = jnp.sum(place[s].astype(full) * marks[where, 1:2], axis=0, keepdims=True)
        c_sum[s] = jnp.broadcast_to(line, (8, rows))
        for copy in out_copies(s):
            copy.start()
        return 0

    lax.fori_loop(0, members, gather, 0)
    for s in (members - 2, members - 1):
        for copy in out_copies(s):
            copy.wait()
    for f in range(1, tiles.count):
        for copy in stage_copies(f):
            copy.wait()
    home.arrive()
    incoming.sent()
    home.sent()


def expert_call(grps, exps, cap, order, routes, comb_all, n_all, cot_all, both_w, down_w, in_low, down_slab):
    members, rows, width = n_all.shape
    reps = grps * QUAD
    tiles = Tiles(down_slab.shape[0], reps)
    size = tiles.size
    slab, both_hidden = in_low.shape
    units = down_slab.shape[0]
    slots = exps * cap
    shape = jax.ShapeDtypeStruct
    vmem = pl.BlockSpec(memory_space=pltpu.VMEM)
    smem = pl.BlockSpec(memory_space=pltpu.SMEM)
    hbm = pl.BlockSpec(memory_space=pl.ANY)
    results = [
        (shape((members, rows, width), low), hbm),
        (shape((members, rows, width), low), hbm),
        (shape((members, 8, rows), full), vmem),
        (shape((2, width, 2 * size), low), hbm),
        (shape((2, size, width), low), hbm),
        (shape((grps, slab, both_hidden), low), hbm),
        (shape((grps, units, width), low), hbm),
    ]
    dma = pltpu.SemaphoreType.DMA
    return pl.pallas_call(
        functools.partial(expert_kernel, grps, exps, cap),
        out_shape=[r[0] for r in results],
        in_specs=[smem] + [vmem] * 2 + [hbm] * 6,
        out_specs=[r[1] for r in results],
        scratch_shapes=[
            pltpu.VMEM((members, cap, rows), low),
            pltpu.VMEM((QUAD * slots, 128), full),
            pltpu.VMEM((QUAD * slots, width), low),
            pltpu.VMEM((QUAD * slots, width), low),
            pltpu.VMEM((tiles.count, width, 2 * size), low),
            pltpu.VMEM((tiles.count, size, width), low),
            pltpu.VMEM((2, exps, rows, width), low),
            pltpu.VMEM((2, exps, rows, width), low),
            pltpu.VMEM((QUAD * slots, width), low),
            pltpu.VMEM((QUAD * slots, width), full),
            pltpu.VMEM((QUAD * slots, 2 * size), low),
            pltpu.VMEM((QUAD * slots, size), low),
            pltpu.VMEM((tiles.count, width, 2 * size), low),
            pltpu.VMEM((tiles.count, size, width), low),
            pltpu.VMEM((2, rows, width), low),
            pltpu.VMEM((2, rows, width), low),
            dma((2, 2)),
            dma((2, 2)),
            dma((2, 2)),
            dma((2, 2 * reps)),
            dma((2, reps + 1)),
            dma((2, 2 * reps)),
            dma((2, max(QUAD, grps))),
            dma((2, tiles.count)),
        ],
        compiler_params=pltpu.CompilerParams(
            collective_id=2, has_side_effects=True, vmem_limit_bytes=60 * 1024 * 1024
        ),
        name="experts",
    )(order, routes, comb_all, n_all, cot_all, both_w, down_w, in_low, down_slab)


class Halving:
    def __init__(self, at, source, kept, bufs, sems, load_sem):
        self.at, self.source, self.kept, self.bufs = at, source, kept, bufs
        self.sems, self.load_sem = sems, load_sem
        self.plane = at.quad * at.exps + at.exp
        self.places = bits_of(QUAD * at.exps)
        self.chip_bits = list(range(self.places - 1))
        self.parts = column_parts(source.shape[2])
        self.orders = [self.chip_bits[c:] + self.chip_bits[:c] for c in range(3)]

    def device(self, bit):
        other = flipped(self.plane, bit)
        return (self.at.grp, other // self.at.exps, other % self.at.exps)

    def first(self):
        core = self.plane % 2
        count = 1 << (self.places - 1)
        device = self.device(0)

        def copies(j):
            return send(
                self.source.at[2 * j + 1 - core], self.bufs[0].at[j], self.sems.at[0, 0, j], self.sems.at[0, 1, j], device
            )

        def load(j):
            return pltpu.make_async_copy(self.source.at[2 * j + core], self.kept.at[j], self.load_sem.at[j])

        return count, copies, load

    def start_first(self):
        count, copies, load = self.first()

        def one(j, _):
            copies(j).start()
            load(j).start()
            return 0

        lax.fori_loop(0, count, one, 0)

    def add_first(self):
        count, copies, load = self.first()

        def one(j, _):
            arrived(self.bufs[0].at[j], self.sems.at[0, 1, j])
            load(j).wait()
            self.bufs[0][j] = (self.bufs[0][j].astype(full) + self.kept[j].astype(full)).astype(low)
            return 0

        lax.fori_loop(0, count, one, 0)

    def hop(self, step, part):
        order = self.orders[part]
        bit = order[step]
        left = [b for b in self.chip_bits if b not in order[:step]]
        pos = left.index(bit)
        half = 1 << (len(left) - 1)
        mine = (self.plane // (1 << (bit + 1))) % 2
        device = self.device(bit + 1)
        begin, size = self.parts[part]
        cols = pl.ds(begin, size)
        base = self.base(step, part)

        def index(j, value):
            return (j >> pos) * (1 << (pos + 1)) + value * (1 << pos) + j % (1 << pos)

        pairs = []
        for j in range(half):
            copy = functools.partial(
                send,
                self.bufs[step].at[index(j, 1 - mine), :, cols],
                self.bufs[step + 1].at[j, :, cols],
                self.sems.at[1, 0, base + j],
                self.sems.at[1, 1, base + j],
                device,
            )
            pairs.append((copy, index(j, mine), j))
        return pairs, begin, size, base

    def base(self, step, part):
        n = len(self.chip_bits)
        return part * (1 << n) + sum(1 << (n - 1 - s) for s in range(step))

    def start(self, step, part=None):
        for p in range(3) if part is None else [part]:
            for copy, _, _ in self.hop(step, p)[0]:
                copy().start()

    def add(self, step, part):
        pairs, begin, size, base = self.hop(step, part)
        cols = pl.ds(begin, size)
        here, there = self.bufs[step], self.bufs[step + 1]
        for _, keep, j in pairs:
            arrived(there.at[j, :, cols], self.sems.at[1, 1, base + j])
            there[j, :, begin : begin + size] = (
                there[j, :, begin : begin + size].astype(full) + here[keep, :, begin : begin + size].astype(full)
            ).astype(low)

    def next(self, step):
        for p in range(3):
            self.add(step, p)
            if step + 1 < len(self.chip_bits):
                self.start(step + 1, p)

    def result(self):
        return self.bufs[len(self.chip_bits)]

    def finish(self):
        count, copies, _ = self.first()

        def one(j, _):
            copies(j).wait_send()
            return 0

        lax.fori_loop(0, count, one, 0)
        for step in range(len(self.chip_bits)):
            for p in range(3):
                for copy, _, _ in self.hop(step, p)[0]:
                    copy().wait_send()


def backward_kernel(
    grps,
    exps,
    lengths,
    deal,
    rel_bias,
    n_parts,
    y_parts,
    c_parts,
    both_g,
    down_g,
    in_before,
    down_before,
    n1_in,
    routes_col,
    tokens,
    gains,
    router,
    h1_in,
    n2_in,
    g_in,
    probs_in,
    qkv,
    lse,
    mine,
    wqkv,
    wout,
    token_grad,
    block_out,
    small_out,
    in_parts,
    down_parts,
    qkv_parts,
    out_parts,
    kept,
    n_bufs,
    y_bufs,
    c_in,
    dh1,
    dz_send,
    dz_all,
    do_send,
    do_in,
    bias,
    bias_sum,
    dqkv,
    dn1_send,
    dn1_in,
    n1,
    wq_send,
    og_send,
    blk_send,
    blk_in,
    small_send,
    small_exp,
    small_sum,
    small_rep,
    n_sem,
    y_sem,
    load_sem,
    c_sem,
    weight_sem,
    down_sem,
    dz_sem,
    do_sem,
    dn1_sem,
    wq_sem,
    og_sem,
    blk_sem,
    small_sem,
    small2_sem,
    n1_sem,
):
    at = Where(grps, exps)
    reps = at.reps
    rows, width = tokens.shape
    heads = HEADS // exps
    head_dim = width // HEADS
    head_cols = heads * head_dim
    block_cols = min(128, head_cols)
    row_block = wqkv.shape[2]
    out_cols = wout.shape[3]
    tiles = Tiles(down_parts.shape[1], reps)
    scale = 1.0 / math.sqrt(head_dim)
    SEND, RECV = 0, 1
    plane = at.quad * exps + at.exp
    members = QUAD * exps

    def exp_peer(k):
        return (at.exp + k) % exps

    greet_all(at)

    dn = Halving(at, n_parts, kept, n_bufs, n_sem, load_sem.at[0])
    ys = Halving(at, y_parts, kept, y_bufs, y_sem, load_sem.at[1])
    dn.start_first()
    homes = [
        Homeward(
            at, tiles, t + 1, both_g.at[t], down_g.at[t], in_parts, down_parts, weight_sem.at[t], down_sem.at[t]
        )
        for t in range(2)
    ]
    homes[0].start()
    n1_copy = pltpu.make_async_copy(n1_in, n1, n1_sem)
    n1_copy.start()

    def c_copy(k):
        other = (plane + k) % members
        return other, send(
            c_parts.at[other],
            c_in.at[plane],
            c_sem.at[SEND, other],
            c_sem.at[RECV, plane],
            (at.grp, other // exps, other % exps),
        )

    def start_c(k, _):
        c_copy(k)[1].start()
        return 0

    lax.fori_loop(1, members, start_c, 0)
    pltpu.make_async_copy(c_parts.at[plane], c_in.at[plane], c_sem.at[RECV, plane]).start()

    span = 2 * rows
    bucket = bucket_of(lane_of((8, span)) - rows)
    for h in range(heads):
        line = jnp.zeros((8, span), full)
        for b in range(BUCKETS):
            line = jnp.where(bucket == b, rel_bias[b, at.exp * heads + h], line)
        whole = jnp.broadcast_to(line[0:1], (rows, span))
        bias[h] = pltpu.roll(whole, 0, 1, stride=1, stride_axis=0)[:, rows:]

    dn.add_first()
    dn.start(0)
    ys.start_first()

    def wait_c(k, _):
        arrived(c_in.at[k], c_sem.at[RECV, k])
        return 0

    lax.fori_loop(0, members, wait_c, 0)
    lane = lane_of((rows, 128))
    comb_rows = []
    for e in range(exps):
        total = c_in[e]
        for q in range(1, QUAD):
            total = total + c_in[q * exps + e]
        comb_rows.append(total[0:1, :])
    comb_rows.append(jnp.zeros((128 - exps, rows), full))
    comb_grad = jnp.concatenate(comb_rows, axis=0).T
    valid = row_of((rows, 1)) < lengths[at.me]
    probs = probs_in[...]
    hot = jnp.logical_or(lane == routes_col[:, 0:1], lane == routes_col[:, 1:2])
    picked = jnp.where(hot, probs, 0.0)
    total = jnp.sum(picked, axis=1, keepdims=True)
    gate = picked / total
    gate_grad_rows = jnp.where(valid, comb_grad, 0.0)
    spread_grad = jnp.sum(gate_grad_rows * gate, axis=1, keepdims=True)
    probs_grad = jnp.where(hot, (gate_grad_rows - spread_grad) / total, 0.0)
    logit_grad = probs * (probs_grad - jnp.sum(probs_grad * probs, axis=1, keepdims=True))
    n2 = n2_in[...].astype(full)
    router_rows = lax.dot_general(
        logit_grad, n2, (((0,), (0,)), ((), ())), preferred_element_type=full, precision=highest
    )
    small_rows = small_send.shape[0]
    small_send[...] = jnp.zeros_like(small_send)
    small_send[0:exps, :] = router_rows[0:exps, :]
    router_back = nt(logit_grad, router[...], precision=highest)
    h1 = h1_in[...]
    r2 = lax.rsqrt(jnp.mean(h1 * h1, axis=1, keepdims=True) + eps_norm)

    dn.next(0)
    ys.add_first()
    dn.next(1)
    steps = len(dn.chip_bits)
    for step in range(2, steps):
        dn.next(step)

    n2_grad = router_back + dn.result()[0].astype(full)
    scaled = n2_grad * gains[1:2, :]
    hidden_grad = (
        g_in[...].astype(full)
        + r2 * scaled
        - h1 * (r2 * r2 * r2) * jnp.mean(scaled * h1, axis=1, keepdims=True)
    )
    dh1[...] = hidden_grad
    small_send[exps + 1 : exps + 2, :] = jnp.sum(n2_grad * h1 * r2, axis=0, keepdims=True)
    branch = hidden_grad.astype(low)
    dz_send[...] = branch
    for e in range(exps):
        total = jnp.zeros((rows, row_block), full)
        for r in range(reps):
            total = total + nt(branch[:, r * out_cols : (r + 1) * out_cols], wout[e, r])
        do_send[e] = total.astype(low)

    def do_copies():
        return [
            send(
                do_send.at[exp_peer(k)],
                do_in.at[at.exp],
                do_sem.at[SEND, exp_peer(k)],
                do_sem.at[RECV, at.exp],
                at.device(at.rep, exp_peer(k)),
            )
            for k in range(1, exps)
        ]

    for copy in do_copies():
        copy.start()
    pltpu.make_async_copy(do_send.at[at.exp], do_in.at[at.exp], do_sem.at[RECV, at.exp]).start()

    def dz_copies():
        return [
            send(
                dz_send,
                dz_all.at[at.exp],
                dz_sem.at[SEND, exp_peer(k)],
                dz_sem.at[RECV, at.exp],
                at.device(at.rep, exp_peer(k)),
            )
            for k in range(1, exps)
        ]

    for copy in dz_copies():
        copy.start()
    dz_all[at.exp] = branch
    homes[1].start()
    ys.start(0)

    bias_sum[...] = jnp.zeros_like(bias_sum)

    def attend_back(i, _):
        s = (at.exp + 1 + i) % exps
        arrived(do_in.at[s], do_sem.at[RECV, s])
        ok = lane_of((rows, rows)) < lengths[at.base + s]
        block_lane = lane_of((rows, block_cols))
        for c in range(head_cols // block_cols):
            cols = slice(c * block_cols, (c + 1) * block_cols)
            k_cols = slice(head_cols + c * block_cols, head_cols + (c + 1) * block_cols)
            v_cols = slice(2 * head_cols + c * block_cols, 2 * head_cols + (c + 1) * block_cols)
            q = qkv[s, :, cols]
            k = qkv[s, :, k_cols]
            v = qkv[s, :, v_cols]
            do = do_in[s, :, cols]
            dq = jnp.zeros((rows, block_cols), full)
            dk = jnp.zeros((rows, block_cols), full)
            dv = jnp.zeros((rows, block_cols), full)
            for t in range(block_cols // head_dim):
                h = c * (block_cols // head_dim) + t
                here = jnp.logical_and(block_lane >= t * head_dim, block_lane < (t + 1) * head_dim)
                zero = jnp.zeros_like(q)
                q_h = jnp.where(here, q, zero)
                do_h = jnp.where(here, do, zero)
                scores = nt(q_h, k) * scale + bias[h]
                total = jnp.sum(jnp.where(lane == h, lse[s], 0.0), axis=1, keepdims=True)
                p = jnp.where(ok, jnp.exp(scores - total), 0.0)
                dp = nt(do_h, v)
                delta = jnp.sum(dp * p, axis=1, keepdims=True)
                ds = (p * (dp - delta)).astype(low)
                bias_sum[h] += ds.astype(full)
                dv = jnp.where(here, tn(p.astype(low), do), dv)
                dq = jnp.where(here, jnp.dot(ds, k, preferred_element_type=full), dq)
                dk = jnp.where(here, tn(ds, q), dk)
            dqkv[s, :, cols] = (dq * scale).astype(low)
            dqkv[s, :, k_cols] = (dk * scale).astype(low)
            dqkv[s, :, v_cols] = dv.astype(low)
        for e in range(exps):
            dn1_send[s, :, e * row_block : (e + 1) * row_block] = jnp.dot(
                dqkv[s], wqkv[e], preferred_element_type=full
            ).astype(low)

        @pl.when(i < exps - 1)
        def _():
            send(
                dn1_send.at[s], dn1_in.at[at.exp], dn1_sem.at[SEND, s], dn1_sem.at[RECV, at.exp], at.device(at.rep, s)
            ).start()

        @pl.when(i == exps - 1)
        def _():
            pltpu.make_async_copy(dn1_send.at[s], dn1_in.at[at.exp], dn1_sem.at[RECV, at.exp]).start()

        return 0

    lax.fori_loop(0, exps, attend_back, 0)

    n1_copy.wait()
    seg = wq_send.shape[2]
    segs = qkv_parts.shape[1]
    parts = wq_send.shape[1]
    for e in range(exps):
        total = jnp.zeros((3 * head_cols, row_block), full)
        for s in range(exps):
            total = total + tn(dqkv[s], n1[s, :, e * row_block : (e + 1) * row_block])
        for j in range(parts):
            wq_send[e, j] = total[j * seg : (j + 1) * seg].astype(low)

    def owner(j):
        section, within = j // (head_cols // seg), j % (head_cols // seg)
        col = section * width + at.exp * head_cols + within * seg
        block = col // seg
        return block // segs, block % segs

    def wq_copy(i):
        e, j = i // parts, i % parts
        rep, k = owner(j)
        dst = qkv_parts.at[at.rep, k]
        recv = wq_sem.at[RECV, at.rep * segs + k]
        stays = jnp.logical_and(rep == at.rep, e == at.exp)
        return (
            stays,
            functools.partial(send, wq_send.at[e, j], dst, wq_sem.at[SEND, i], recv, at.device(rep, e)),
            functools.partial(pltpu.make_async_copy, wq_send.at[e, j], dst, recv),
        )

    def start_wq(i, _):
        stays, away, local = wq_copy(i)

        @pl.when(stays)
        def _():
            local().start()

        @pl.when(jnp.logical_not(stays))
        def _():
            away().start()

        return 0

    lax.fori_loop(0, exps * parts, start_wq, 0)
    for k in range(1, exps):
        arrived(dz_all.at[exp_peer(k)], dz_sem.at[RECV, exp_peer(k)])
    for r in range(reps):
        total = jnp.zeros((head_cols, out_cols), full)
        for s in range(exps):
            total = total + tn(mine[s], dz_all[s, :, r * out_cols : (r + 1) * out_cols])
        og_send[r] = total.astype(low)

    def og_copies():
        return [
            send(
                og_send.at[(at.rep + k) % reps],
                out_parts.at[at.rep],
                og_sem.at[SEND, (at.rep + k) % reps],
                og_sem.at[RECV, at.rep],
                at.device((at.rep + k) % reps, at.exp),
            )
            for k in range(1, reps)
        ]

    for copy in og_copies():
        copy.start()
    pltpu.make_async_copy(og_send.at[at.rep], out_parts.at[at.rep], og_sem.at[RECV, at.rep]).start()

    line_lane = lane_of((8, 128))
    line_row = row_of((8, 128))
    bias_line = jnp.zeros((8, 128), full)
    flip = jnp.where(row_of((rows, rows)) + lane_of((rows, rows)) == rows - 1, 1.0, 0.0)
    turned_bucket = bucket_of(rows - 1 - lane_of((8, span)))
    for h in range(heads):
        flipped = jnp.dot(bias_sum[h], flip, precision=highest, preferred_element_type=full)
        square = jnp.concatenate([flipped, jnp.zeros((rows, rows), full)], axis=1)
        turned = pltpu.roll(square, 0, 1, stride=1, stride_axis=0)
        sums = jnp.broadcast_to(jnp.sum(turned, axis=0, keepdims=True), (8, span))
        for b in range(BUCKETS):
            value = jnp.sum(jnp.where(turned_bucket == b, sums, 0.0), axis=1, keepdims=True)
            bias_line = jnp.where(jnp.logical_and(line_row == h, line_lane == b), value, bias_line)
    for h in range(heads):
        small_send[exps + 2 : exps + 3, h * 128 : (h + 1) * 128] = bias_line[h : h + 1, :]

    ys.next(0)

    for e in range(exps):
        arrived(dn1_in.at[e], dn1_sem.at[RECV, e])
    n1_grad = dn1_in[0].astype(full)
    for e in range(1, exps):
        n1_grad = n1_grad + dn1_in[e].astype(full)
    x = tokens[...].astype(full)
    r1 = lax.rsqrt(jnp.mean(x * x, axis=1, keepdims=True) + eps_norm)
    scaled = n1_grad * gains[0:1, :]
    token_grad[...] = (
        dh1[...] + r1 * scaled - x * (r1 * r1 * r1) * jnp.mean(scaled * x, axis=1, keepdims=True)
    )
    small_send[exps : exps + 1, :] = jnp.sum(n1_grad * x * r1, axis=0, keepdims=True)

    def small_copies():
        return [
            send(
                small_send,
                small_exp.at[at.exp],
                small_sem.at[SEND, exp_peer(k)],
                small_sem.at[RECV, at.exp],
                at.device(at.rep, exp_peer(k)),
            )
            for k in range(1, exps)
        ]

    for copy in small_copies():
        copy.start()
    small_exp[at.exp] = small_send[...]
    for step in range(1, steps):
        ys.next(step)
    block = jnp.where(valid, h1_in[...] + ys.result()[0].astype(full), 0.0).astype(low)
    blk_send[...] = block

    def blk_copies():
        return [
            send(
                blk_send,
                blk_in.at[at.exp],
                blk_sem.at[SEND, exp_peer(k)],
                blk_sem.at[RECV, at.exp],
                at.device(at.rep, exp_peer(k)),
            )
            for k in range(1, exps)
        ]

    for copy in blk_copies():
        copy.start()
    blk_in[at.exp] = block
    for k in range(1, exps):
        arrived(small_exp.at[exp_peer(k)], small_sem.at[RECV, exp_peer(k)])
    total = small_exp[0]
    for e in range(1, exps):
        total = total + small_exp[e]
    small_sum[0] = total
    for e in range(exps):
        small_sum[0, exps + 3 + e : exps + 4 + e, :] = small_exp[e, exps + 2 : exps + 3, :]

    def small2_copies():
        return [
            send(
                small_sum.at[0],
                small_rep.at[at.rep],
                small2_sem.at[SEND, (at.rep + k) % reps],
                small2_sem.at[RECV, at.rep],
                at.device((at.rep + k) % reps, at.exp),
            )
            for k in range(1, reps)
        ]

    for copy in small2_copies():
        copy.start()
    small_rep[at.rep] = small_sum[0]
    for k in range(1, exps):
        arrived(blk_in.at[exp_peer(k)], blk_sem.at[RECV, exp_peer(k)])
    chosen = jnp.zeros((rows, width), full)
    for e in range(exps):
        chosen = jnp.where(deal[at.base + e] == at.me, blk_in[e].astype(full), chosen)
    block_out[...] = chosen.astype(low)
    for k in range(1, reps):
        arrived(small_rep.at[(at.rep + k) % reps], small2_sem.at[RECV, (at.rep + k) % reps])
    total = small_rep[0]
    for r in range(1, reps):
        total = total + small_rep[r]
    small_out[...] = total

    for home in homes:
        home.arrive()
    for r in range(reps):
        arrived(out_parts.at[r], og_sem.at[RECV, r])

    def wq_in(i, _):
        arrived(qkv_parts.at[i // segs, i % segs], wq_sem.at[RECV, i])
        return 0

    lax.fori_loop(0, reps * segs, wq_in, 0)

    def sent_c(k, _):
        c_copy(k)[1].wait_send()
        return 0

    lax.fori_loop(1, members, sent_c, 0)
    dn.finish()
    ys.finish()

    for home in homes:
        home.sent()

    def sent_wq(i, _):
        stays, away, _ = wq_copy(i)

        @pl.when(jnp.logical_not(stays))
        def _():
            away().wait_send()

        return 0

    lax.fori_loop(0, exps * parts, sent_wq, 0)
    for copies in (
        do_copies(),
        dz_copies(),
        og_copies(),
        small_copies(),
        blk_copies(),
        small2_copies(),
    ):
        for copy in copies:
            copy.wait_send()
    for k in range(1, exps):
        arrived(dn1_send.at[exp_peer(k)], dn1_sem.at[SEND, exp_peer(k)])


def backward_call(
    grps, exps, lengths, deal, rel_bias, n_parts, y_parts, c_parts, both_g, down_g, in_before, down_before, n1, routes_col,
    tokens, gains, router, h1, n2, g, probs, qkv, lse, mine, wqkv, wout
):
    reps = grps * QUAD
    rows, width = tokens.shape
    heads = HEADS // exps
    head_cols = width // exps
    row_block = wqkv.shape[2]
    out_cols = wout.shape[3]
    shard_cols = 3 * width // reps
    seg = math.gcd(shard_cols, head_cols)
    segs = shard_cols // seg
    parts = 3 * head_cols // seg
    members = QUAD * exps
    chip_bits = bits_of(members) - 1
    small_rows = -(-(2 * exps + 3) // 8) * 8
    shape = jax.ShapeDtypeStruct
    vmem = pl.BlockSpec(memory_space=pltpu.VMEM)
    smem = pl.BlockSpec(memory_space=pltpu.SMEM)
    hbm = pl.BlockSpec(memory_space=pl.ANY)
    results = [
        (shape((rows, width), full), vmem),
        (shape((rows, width), low), vmem),
        (shape((small_rows, width), full), vmem),
        (shape(in_before.shape, low), hbm),
        (shape(down_before.shape, low), hbm),
        (shape((reps, segs, seg, row_block), low), hbm),
        (shape((reps, row_block, out_cols), low), hbm),
    ]
    dma = pltpu.SemaphoreType.DMA
    bufs = [pltpu.VMEM((1 << (chip_bits - s), rows, width), low) for s in range(chip_bits + 1)]
    return pl.pallas_call(
        functools.partial(backward_kernel, grps, exps),
        out_shape=[r[0] for r in results],
        in_specs=[smem] * 3 + [hbm] * 8 + [vmem] * 13,
        out_specs=[r[1] for r in results],
        scratch_shapes=[
            pltpu.VMEM((members // 2, rows, width), low),
            list(bufs),
            list(bufs),
            pltpu.VMEM((members, 8, rows), full),
            pltpu.VMEM((rows, width), full),
            pltpu.VMEM((rows, width), low),
            pltpu.VMEM((exps, rows, width), low),
            pltpu.VMEM((exps, rows, head_cols), low),
            pltpu.VMEM((exps, rows, head_cols), low),
            pltpu.VMEM((heads, rows, rows), full),
            pltpu.VMEM((heads, rows, rows), full),
            pltpu.VMEM((exps, rows, 3 * head_cols), low),
            pltpu.VMEM((exps, rows, width), low),
            pltpu.VMEM((exps, rows, width), low),
            pltpu.VMEM((exps, rows, width), low),
            pltpu.VMEM((exps, parts, seg, row_block), low),
            pltpu.VMEM((reps, row_block, out_cols), low),
            pltpu.VMEM((rows, width), low),
            pltpu.VMEM((exps, rows, width), low),
            pltpu.VMEM((small_rows, width), full),
            pltpu.VMEM((exps, small_rows, width), full),
            pltpu.VMEM((1, small_rows, width), full),
            pltpu.VMEM((reps, small_rows, width), full),
            dma((2, 2, 3 << chip_bits)),
            dma((2, 2, 3 << chip_bits)),
            dma((2, members // 2)),
            dma((2, members)),
            dma((2, 2, 2 * reps)),
            dma((2, 2, max(QUAD, grps))),
            dma((2, exps)),
            dma((2, exps)),
            dma((2, exps)),
            dma((2, max(exps * parts, reps * segs))),
            dma((2, reps)),
            dma((2, exps)),
            dma((2, exps)),
            dma((2, reps)),
            dma,
        ],
        compiler_params=pltpu.CompilerParams(
            collective_id=1, has_side_effects=True, vmem_limit_bytes=60 * 1024 * 1024
        ),
        input_output_aliases={8: 3, 9: 4},
        name="backward",
    )(
        lengths, deal, rel_bias, n_parts, y_parts, c_parts, both_g, down_g, in_before, down_before, n1, routes_col, tokens,
        gains, router, h1, n2, g, probs, qkv, lse, mine, wqkv, wout
    )


def per_device(
    tokens,
    cotangent,
    seq_lengths,
    deal,
    routes,
    attn_qkv,
    qkv_first,
    qkv_second,
    attn_out,
    out_first,
    out_second,
    rel_bias,
    bias_first,
    bias_second,
    router,
    router_first,
    router_second,
    norm_gains,
    gains_first,
    gains_second,
    expert_in,
    in_first,
    in_second,
    expert_out,
    down_first,
    down_second,
):
    rows, width = tokens.shape
    experts = router.shape[1]
    capacity = (10 * rows + 4 * experts - 1) // (4 * experts)
    exps = lax.axis_size("exp")
    grps = lax.axis_size("grp")
    heads = HEADS // exps
    place = lax.axis_index("exp")
    quad = lax.axis_index("quad")
    base = lax.axis_index(REP) * exps
    me = base + place
    row_block = attn_qkv.shape[0]
    members = QUAD * exps

    my_routes = lax.dynamic_slice_in_dim(routes, me * rows, rows, 0)
    routes_col = jnp.zeros((rows, 128), jnp.int32).at[:, :2].set(my_routes)
    gains = jnp.zeros((8, width), full).at[:2].set(norm_gains.T)
    router_wide = jnp.zeros((width, 128), full).at[:, :experts].set(router)
    in_low = expert_in[0].astype(low)
    down_low = expert_out[0].astype(low)
    (
        both_w, down_w, cot_all, n_all, comb_all, qkv, lse, context_mine, normed_group, wqkv, wout,
        hidden_one, normed_two, router_probs,
    ) = forward_call(
        grps, exps, seq_lengths, rel_bias, routes_col, tokens, cotangent, gains, router_wide,
        attn_qkv.astype(low).T, attn_out.astype(low), in_low, down_low,
    )

    plane_base = base - quad * exps
    plane_deal = lax.dynamic_slice_in_dim(deal, plane_base, members, 0) - plane_base
    plane_routes = lax.dynamic_slice_in_dim(routes, plane_base * rows, members * rows, 0)
    plane_routes = jnp.transpose(plane_routes.reshape(QUAD, exps, rows, 2), (0, 3, 1, 2))
    plane_routes = jnp.pad(plane_routes, ((0, 0), (0, 0), (0, 8 - exps), (0, 0)), constant_values=-1)
    n_parts, y_parts, c_parts, both_g, down_g, in_before, down_before = expert_call(
        grps, exps, capacity, plane_deal, plane_routes, comb_all, n_all, cot_all, both_w, down_w, in_low, down_low
    )
    valid_rows = jnp.arange(rows, dtype=jnp.int32) < seq_lengths[me]
    my_cotangent = lax.dynamic_index_in_dim(cot_all, deal[me] - plane_base, 0, keepdims=False)
    my_cotangent = jnp.where(valid_rows[:, None], my_cotangent, jnp.zeros_like(my_cotangent))
    token_grad, block_out, small, in_parts, down_parts, qkv_parts, out_parts = backward_call(
        grps, exps, seq_lengths, deal, rel_bias, n_parts, y_parts, c_parts, both_g, down_g, in_before,
        down_before, normed_group, routes_col, tokens, gains, router_wide, hidden_one, normed_two, my_cotangent, router_probs,
        qkv, lse, context_mine, wqkv, wout,
    )
    down_share = jnp.sum(down_parts.astype(full), axis=0)[None]
    in_share = jnp.sum(in_parts.astype(full), axis=0)[None]
    qkv_share = jnp.sum(qkv_parts.astype(full), axis=0).reshape(-1, row_block).T
    out_share = jnp.sum(out_parts.astype(full), axis=0)
    router_total = small[:experts].T
    gains_total = small[exps : exps + 2].T
    bias_total = jnp.transpose(
        small[exps + 3 : 2 * exps + 3, : heads * 128].reshape(exps, heads, 128)[:, :, :BUCKETS], (2, 0, 1)
    ).reshape(BUCKETS, HEADS)

    qkv_new = adamw_update(attn_qkv, qkv_first, qkv_second, qkv_share, 1.5 / math.sqrt(D), 0.1)
    out_new = adamw_update(attn_out, out_first, out_second, out_share, 6.0 / math.sqrt(D), 0.1)
    bias_new = adamw_update(rel_bias, bias_first, bias_second, bias_total, 0.3, 0.0)
    router_new = adamw_update(
        router, router_first, router_second, router_total, 1.0 / math.sqrt(D), 0.1
    )
    gains_new = adamw_update(norm_gains, gains_first, gains_second, gains_total, 0.5, 0.0)
    in_new = adamw_update(expert_in, in_first, in_second, in_share, 1.5 / math.sqrt(D), 0.1)
    down_new = adamw_update(
        expert_out, down_first, down_second, down_share, 1.5 / math.sqrt(FF), 0.1
    )
    return (
        (block_out, token_grad)
        + qkv_new
        + out_new
        + bias_new
        + router_new
        + gains_new
        + in_new
        + down_new
    )


def bucket_onehot(length):
    places = jnp.arange(length, dtype=jnp.int32)
    offset = places[None, :] - places[:, None]
    distance = jnp.abs(offset)
    bucket = 16 * (offset > 0).astype(jnp.int32)
    for threshold in thresholds:
        bucket = bucket + (distance >= threshold).astype(jnp.int32)
    return (bucket[:, :, None] == jnp.arange(BUCKETS, dtype=jnp.int32)[None, None, :]).astype(full)


def swap(pieces, axes):
    return lax.all_to_all(pieces, axes, split_axis=0, concat_axis=0, tiled=True)


def spread(block, axes):
    members = lax.axis_size(axes)
    return swap(jnp.broadcast_to(block[None], (members,) + block.shape), axes)


def plain_device(
    tokens,
    cotangent,
    seq_lengths,
    deal,
    routes,
    attn_qkv,
    qkv_first,
    qkv_second,
    attn_out,
    out_first,
    out_second,
    rel_bias,
    bias_first,
    bias_second,
    router,
    router_first,
    router_second,
    norm_gains,
    gains_first,
    gains_second,
    expert_in,
    in_first,
    in_second,
    expert_out,
    down_first,
    down_second,
):
    rows, width = tokens.shape
    head_dim = width // HEADS
    score_scale = 1.0 / math.sqrt(head_dim)
    experts = router.shape[1]
    capacity = (10 * rows + 4 * experts - 1) // (4 * experts)
    exps = lax.axis_size("exp")
    grps = lax.axis_size("grp")
    reps = grps * QUAD
    heads = HEADS // exps
    head_cols = heads * head_dim
    place = lax.axis_index("exp")
    base = lax.axis_index(REP) * exps
    me = base + place
    slab = expert_in.shape[1]
    units = expert_out.shape[1]
    quarter = grps * units

    row_block = attn_qkv.shape[0]
    qkv_rows = lax.all_gather(attn_qkv.astype(low), REP, axis=1, tiled=True)
    out_rows = lax.all_gather(attn_out.astype(low), REP, axis=1, tiled=True)
    qkv_pieces = jnp.transpose(
        qkv_rows.reshape(row_block, 3, exps, head_cols), (2, 0, 1, 3)
    ).reshape(exps, row_block, 3 * head_cols)
    qkv_mine = swap(qkv_pieces, "exp").reshape(width, 3 * head_cols)
    full_out = spread(out_rows, "exp").reshape(width, width)

    group_tokens = spread(tokens, "exp")
    group_cotangent = spread(cotangent, "exp")
    my_cotangent = lax.dynamic_index_in_dim(group_cotangent, deal[me] - base, 0, keepdims=False)

    my_routes = lax.dynamic_slice_in_dim(routes, me * rows, rows, 0)
    places = jnp.arange(rows, dtype=jnp.int32)
    valid_rows = (places < seq_lengths[me]).astype(full)
    group_lengths = lax.dynamic_slice_in_dim(seq_lengths, base, exps, 0)
    key_ok = places[None, :] < group_lengths[:, None]
    gain_one = norm_gains[:, 0]
    gain_two = norm_gains[:, 1]

    chosen = (my_routes[:, :, None] == jnp.arange(experts, dtype=jnp.int32)[None, None, :]).astype(full)
    flat_routes = my_routes.reshape(-1)
    route_hot = (flat_routes[:, None] == jnp.arange(experts, dtype=jnp.int32)[None, :]).astype(jnp.int32)
    before = jnp.cumsum(route_hot, axis=0) - route_hot
    slot_index = jnp.sum(before * route_hot, axis=-1)
    target = (flat_routes * capacity + slot_index).reshape(rows, 2)
    slots = experts * capacity
    slot_ids = jnp.arange(slots, dtype=jnp.int32)
    place_first = slot_ids[:, None] == target[None, :, 0]
    place_second = slot_ids[:, None] == target[None, :, 1]
    place_any = jnp.logical_or(place_first, place_second).astype(low)

    shard_in = expert_in[0].astype(low).reshape(slab, 2, grps, QUAD, units)
    in_pieces = jnp.transpose(shard_in, (1, 3, 0, 2, 4)).reshape(2, 1, QUAD, slab, quarter)
    in_pieces = jnp.broadcast_to(in_pieces, (2, grps, QUAD, slab, quarter)).reshape(
        2, reps, slab, quarter
    )
    down_mine = spread(expert_out[0].astype(low), "grp").reshape(quarter, width)
    gate_mine = swap(in_pieces[0], REP).reshape(width, quarter)
    up_mine = swap(in_pieces[1], REP).reshape(width, quarter)

    upstream = my_cotangent.astype(full) * valid_rows[:, None]

    def to_experts(block):
        sent = block.reshape((1, experts) + block.shape[1:])
        sent = jnp.broadcast_to(sent, (QUAD,) + sent.shape[1:])
        return swap(sent.reshape((QUAD * experts,) + block.shape[1:]), PLANE)

    def dispatch(values):
        return dot(place_any, values).astype(low).reshape(experts, capacity, width)

    expert_upstream = to_experts(dispatch(upstream.astype(low))).reshape(-1, width)
    active_grad_bare = lax.dot_general(
        expert_upstream, down_mine, (((1,), (1,)), ((), ())), preferred_element_type=full
    )

    x_group = group_tokens.astype(full)
    scale_group = lax.rsqrt(jnp.mean(x_group * x_group, axis=-1, keepdims=True) + eps_norm)
    normed_group = (x_group * scale_group * gain_one).astype(low).reshape(exps * rows, width)
    qkv = dot(normed_group, qkv_mine).astype(low).reshape(exps, rows, 3, heads, head_dim)
    queries = qkv[:, :, 0]
    key_rows = qkv[:, :, 1]
    values = qkv[:, :, 2]
    onehot = bucket_onehot(rows)
    bias_mine = lax.dynamic_slice_in_dim(rel_bias, place * heads, heads, 1)
    bias_table = jnp.einsum("ijb,bh->hij", onehot, bias_mine, precision=highest)

    def scores_of():
        raw = (
            jnp.einsum("sihd,sjhd->shij", queries, key_rows, preferred_element_type=full)
            * score_scale
            + bias_table[None]
        )
        return jnp.where(key_ok[:, None, None, :], raw, -1e30)

    scores = scores_of()
    row_max = jnp.max(scores, axis=-1, keepdims=True)
    log_total = row_max + jnp.log(jnp.sum(jnp.exp(scores - row_max), axis=-1, keepdims=True))
    weights_low = jnp.exp(scores - log_total).astype(low)
    context_mine = (
        jnp.einsum("shij,sjhd->sihd", weights_low, values, preferred_element_type=full)
        .astype(low)
        .reshape(exps, rows, head_cols)
    )
    context = jnp.transpose(swap(context_mine, "exp"), (1, 0, 2)).reshape(rows, width)

    x_float = tokens.astype(full)
    scale_one = lax.rsqrt(jnp.mean(x_float * x_float, axis=-1, keepdims=True) + eps_norm)
    hidden_one = x_float + dot(context, full_out)
    scale_two = lax.rsqrt(jnp.mean(hidden_one * hidden_one, axis=-1, keepdims=True) + eps_norm)
    normed_two = (hidden_one * scale_two * gain_two).astype(low)
    normed_float = normed_two.astype(full)
    router_probs = jax.nn.softmax(jnp.dot(normed_float, router, precision=highest), axis=-1)
    picked = jnp.sum(router_probs[:, None, :] * chosen, axis=-1)
    gate_total = jnp.sum(picked, axis=-1, keepdims=True)
    gate_value = picked / gate_total
    combine = gate_value * valid_rows[:, None]
    combine_slots = jnp.sum(
        jnp.where(place_first, combine[None, :, 0], 0.0)
        + jnp.where(place_second, combine[None, :, 1], 0.0),
        axis=1,
    ).reshape(experts, 1, capacity)

    expert_rows = to_experts(dispatch(normed_two)).reshape(-1, width)
    expert_combine = to_experts(combine_slots).reshape(-1, 1)

    gate_part = dot(expert_rows, gate_mine)
    up_part = dot(expert_rows, up_mine)
    active_float, active_pull = jax.vjp(gated_unit, gate_part, up_part)
    active = active_float.astype(low)
    active_scaled = (active_float * expert_combine).astype(low)
    combine_grad_part = jnp.sum(active_float * active_grad_bare, axis=-1).reshape(
        QUAD * experts, 1, capacity
    )
    gate_part_grad, up_part_grad = active_pull(active_grad_bare * expert_combine)
    gate_part_grad = gate_part_grad.astype(low)
    up_part_grad = up_part_grad.astype(low)
    rows_grad_part = (
        lax.dot_general(gate_part_grad, gate_mine, (((1,), (1,)), ((), ())), preferred_element_type=full)
        + lax.dot_general(up_part_grad, up_mine, (((1,), (1,)), ((), ())), preferred_element_type=full)
    ).astype(low)
    output_part = dot(active, down_mine).astype(low)

    combine_grad_back = swap(combine_grad_part, PLANE)
    rows_grad_back = swap(rows_grad_part.reshape(QUAD * experts, capacity, width), PLANE)
    output_back = swap(output_part.reshape(QUAD * experts, capacity, width), PLANE)

    def transposed_dot(a, b):
        return lax.dot_general(a, b, (((0,), (0,)), ((), ())), preferred_element_type=full)

    down_grad = transposed_dot(active_scaled, expert_upstream).astype(low)
    gate_grad = transposed_dot(expert_rows, gate_part_grad).astype(low)
    up_grad = transposed_dot(expert_rows, up_part_grad).astype(low)
    down_share = jnp.sum(
        swap(down_grad.reshape(grps, units, width), "grp").astype(full), axis=0
    )[None]

    def in_columns(grad):
        back = swap(grad.reshape(reps, slab, quarter), REP).astype(full)
        back = jnp.sum(back.reshape(grps, QUAD, slab, grps, units), axis=0)
        return jnp.transpose(back, (1, 2, 0, 3)).reshape(slab, grps * QUAD * units)

    in_share = jnp.concatenate([in_columns(gate_grad), in_columns(up_grad)], axis=1)[None]

    def from_slots(placed, parts):
        hot = jnp.broadcast_to(placed.astype(low)[None], (QUAD,) + placed.shape).reshape(-1, rows)
        return lax.dot_general(
            hot, parts.reshape(-1, width), (((0,), (0,)), ((), ())), preferred_element_type=full
        )

    mixture = combine[:, :1] * from_slots(place_first, output_back) + combine[:, 1:] * from_slots(
        place_second, output_back
    )
    block_loader = (valid_rows[:, None] * (hidden_one + mixture)).astype(low)
    seq_ids = jnp.arange(deal.shape[0], dtype=jnp.int32)
    dealt_seq = jnp.sum(jnp.where(deal == me, seq_ids, 0))
    block_out = lax.dynamic_index_in_dim(
        spread(block_loader, "exp"), dealt_seq - base, 0, keepdims=False
    )

    combine_grad_slots = jnp.sum(combine_grad_back.reshape(QUAD, slots), axis=0)
    combine_grad = jnp.stack(
        [
            jnp.sum(jnp.where(place_first, combine_grad_slots[:, None], 0.0), axis=0),
            jnp.sum(jnp.where(place_second, combine_grad_slots[:, None], 0.0), axis=0),
        ],
        axis=1,
    )
    gate_grad_value = combine_grad * valid_rows[:, None]
    picked_grad = (
        gate_grad_value - jnp.sum(gate_grad_value * gate_value, axis=-1, keepdims=True)
    ) / gate_total
    probs_grad = jnp.sum(picked_grad[:, :, None] * chosen, axis=1)
    logit_grad = router_probs * (
        probs_grad - jnp.sum(probs_grad * router_probs, axis=-1, keepdims=True)
    )
    router_grad = jnp.dot(normed_float.T, logit_grad, precision=highest)
    normed_grad = jnp.dot(logit_grad, router.T, precision=highest) + from_slots(
        jnp.logical_or(place_first, place_second), rows_grad_back
    )
    scaled_two = normed_grad * gain_two
    hidden_grad = (
        upstream
        + scale_two * scaled_two
        - hidden_one * scale_two**3 * jnp.mean(scaled_two * hidden_one, axis=-1, keepdims=True)
    )
    gain_two_grad = jnp.sum(normed_grad * hidden_one * scale_two, axis=0)
    branch_grad = hidden_grad.astype(low)
    context_grad = lax.dot_general(
        branch_grad, full_out, (((1,), (1,)), ((), ())), preferred_element_type=full
    ).astype(low)
    context_grad_pieces = jnp.transpose(context_grad.reshape(rows, exps, head_cols), (1, 0, 2))
    context_grad_mine = swap(context_grad_pieces, "exp").reshape(exps, rows, heads, head_dim)
    branch_group = spread(branch_grad, "exp").reshape(exps * rows, width)
    out_grad = transposed_dot(context_mine.reshape(exps * rows, head_cols), branch_group).astype(low)

    scores = scores_of()
    probs_again = jnp.exp(scores - log_total)
    weights_again = probs_again.astype(low)
    values_grad = jnp.einsum(
        "shij,sihd->sjhd", weights_again, context_grad_mine, preferred_element_type=full
    )
    probs_grad_att = jnp.einsum(
        "sihd,sjhd->shij", context_grad_mine, values, preferred_element_type=full
    )
    row_delta = jnp.sum(probs_grad_att * probs_again, axis=-1, keepdims=True)
    scores_grad = (probs_again * (probs_grad_att - row_delta)).astype(low)
    scores_grad_sum = jnp.sum(scores_grad.astype(full), axis=0)
    bias_grad_mine = jnp.einsum("hij,ijb->bh", scores_grad_sum, onehot, precision=highest)
    bias_grad = lax.dynamic_update_slice_in_dim(
        jnp.zeros((BUCKETS, HEADS), full), bias_grad_mine, place * heads, 1
    )
    queries_grad = (
        jnp.einsum("shij,sjhd->sihd", scores_grad, key_rows, preferred_element_type=full)
        * score_scale
    )
    keys_grad = (
        jnp.einsum("shij,sihd->sjhd", scores_grad, queries, preferred_element_type=full)
        * score_scale
    )
    qkv_grad = (
        jnp.stack([queries_grad, keys_grad, values_grad], axis=2)
        .astype(low)
        .reshape(exps * rows, 3 * head_cols)
    )
    normed_one_part = lax.dot_general(
        qkv_grad, qkv_mine, (((1,), (1,)), ((), ())), preferred_element_type=full
    ).astype(low)
    normed_one_grad = jnp.sum(
        swap(normed_one_part.reshape(exps, rows, width), "exp").astype(full), axis=0
    )
    scaled_one = normed_one_grad * gain_one
    token_grad = (
        hidden_grad
        + scale_one * scaled_one
        - x_float * scale_one**3 * jnp.mean(scaled_one * x_float, axis=-1, keepdims=True)
    )
    gain_one_grad = jnp.sum(normed_one_grad * x_float * scale_one, axis=0)

    qkv_weight_grad = transposed_dot(normed_group, qkv_grad).astype(low)
    qkv_grad_rows = swap(qkv_weight_grad.reshape(exps, row_block, 3 * head_cols), "exp")
    qkv_grad_rows = jnp.transpose(
        qkv_grad_rows.reshape(exps, row_block, 3, head_cols), (1, 2, 0, 3)
    ).reshape(row_block, reps, -1)
    qkv_share = jnp.sum(
        swap(jnp.transpose(qkv_grad_rows, (1, 0, 2)), REP).astype(full), axis=0
    )
    out_pieces = jnp.transpose(out_grad.reshape(row_block, reps, -1), (1, 0, 2))
    out_share = jnp.sum(swap(out_pieces, REP).astype(full), axis=0)

    small = jnp.concatenate(
        [
            router_grad.reshape(-1),
            jnp.stack([gain_one_grad, gain_two_grad], axis=1).reshape(-1),
            bias_grad.reshape(-1),
        ]
    ).reshape(-1, 128)
    small_total = jnp.sum(lax.all_gather(small, ALL, axis=0, tiled=False), axis=0).reshape(-1)
    router_total = small_total[: router.size].reshape(router.shape)
    gains_total = small_total[router.size : router.size + norm_gains.size].reshape(norm_gains.shape)
    bias_total = small_total[router.size + norm_gains.size :].reshape(rel_bias.shape)

    qkv_new = adamw_update(attn_qkv, qkv_first, qkv_second, qkv_share, 1.5 / math.sqrt(D), 0.1)
    out_new = adamw_update(attn_out, out_first, out_second, out_share, 6.0 / math.sqrt(D), 0.1)
    bias_new = adamw_update(rel_bias, bias_first, bias_second, bias_total, 0.3, 0.0)
    router_new = adamw_update(
        router, router_first, router_second, router_total, 1.0 / math.sqrt(D), 0.1
    )
    gains_new = adamw_update(norm_gains, gains_first, gains_second, gains_total, 0.5, 0.0)
    in_new = adamw_update(expert_in, in_first, in_second, in_share, 1.5 / math.sqrt(D), 0.1)
    down_new = adamw_update(
        expert_out, down_first, down_second, down_share, 1.5 / math.sqrt(FF), 0.1
    )
    return (
        (block_out, token_grad)
        + qkv_new
        + out_new
        + bias_new
        + router_new
        + gains_new
        + in_new
        + down_new
    )


def solution(mesh):
    reps, exps = mesh.devices.shape
    split = Mesh(mesh.devices.reshape(reps // QUAD, QUAD, exps), ALL)
    by_rows = P(ALL, None)
    attn = P("exp", REP)
    expert = P("exp", REP, None)
    return jax.shard_map(
        per_device if (reps, exps) == (2 * QUAD, 4) else plain_device,
        mesh=split,
        in_specs=(by_rows, by_rows) + (P(),) * 3 + (attn,) * 6 + (P(),) * 9 + (expert,) * 6,
        out_specs=(by_rows, by_rows) + (attn,) * 6 + (P(),) * 9 + (expert,) * 6,
        check_vma=False,
    )
```

```python
import functools
import math

import jax
import jax.numpy as jnp
from jax import lax
from jax.experimental import pallas as pl
from jax.experimental.pallas import tpu as pltpu
from jax.sharding import Mesh
from jax.sharding import PartitionSpec as P

D = 1024
HEADS = 16
FF = 2816
BUCKETS = 32
STEP = 10
QUAD = 4
REP = ("grp", "quad")
PLANE = ("quad", "exp")
ALL = ("grp", "quad", "exp")

highest = lax.Precision.HIGHEST
eps_norm = 1e-06
thresholds = (1, 2, 3, 4, 5, 6, 7, 8, 11, 16, 22, 32, 45, 64, 90)
beta_one = 0.9
beta_two = 0.999
eps_adam = 1e-08
low = jnp.bfloat16
full = jnp.float32
MESH = pl.DeviceIdType.MESH


def adamw_update(weight, moment, second, gradient, step_rate, decay_factor):
    new_moment = beta_one * moment + (1.0 - beta_one) * gradient
    new_second = beta_two * second + (1.0 - beta_two) * gradient * gradient
    corrected = new_moment / (1.0 - beta_one**STEP)
    scaled = new_second / (1.0 - beta_two**STEP)
    new_weight = weight - step_rate * (
        corrected / (jnp.sqrt(scaled) + eps_adam) + decay_factor * weight
    )
    return (new_moment, new_second, new_weight)


def gated_unit(gate_input, up_input):
    return jax.nn.gelu(gate_input, approximate=True) * up_input


def dot(a, b):
    return jnp.dot(a, b, preferred_element_type=full)


def nt(a, b, precision=None):
    return lax.dot_general(a, b, (((1,), (1,)), ((), ())), preferred_element_type=full, precision=precision)


def tn(a, b):
    return lax.dot_general(a, b, (((0,), (0,)), ((), ())), preferred_element_type=full)


class Where:
    def __init__(self, grps, exps):
        self.grps, self.exps = grps, exps
        self.reps = grps * QUAD
        self.grp = lax.axis_index("grp")
        self.quad = lax.axis_index("quad")
        self.exp = lax.axis_index("exp")
        self.rep = self.grp * QUAD + self.quad
        self.base = self.rep * exps
        self.me = self.base + self.exp

    def device(self, rep, exp):
        return (rep // QUAD, rep % QUAD, exp)

    def near(self, flip):
        q = self.quad
        if flip & 1:
            q = q + 1 - 2 * (q % 2)
        if flip & 2:
            q = q + 2 - 4 * (q // 2)
        return q


def send(src, dst, send_sem, recv_sem, device):
    return pltpu.make_async_remote_copy(
        src_ref=src, dst_ref=dst, send_sem=send_sem, recv_sem=recv_sem, device_id=device, device_id_type=MESH
    )


def arrived(ref, sem):
    pltpu.make_async_copy(ref, ref, sem).wait()


def greet_all(at):
    count = at.reps * at.exps
    barrier = pltpu.get_barrier_semaphore()

    def greet(k, _):
        other = (at.me + k) % count
        pl.semaphore_signal(
            barrier, inc=1, device_id=at.device(other // at.exps, other % at.exps), device_id_type=MESH
        )
        return 0

    lax.fori_loop(1, count, greet, 0)
    pl.semaphore_wait(barrier, count - 1)


def lane_of(shape):
    return lax.broadcasted_iota(jnp.int32, shape, 1)


def row_of(shape):
    return lax.broadcasted_iota(jnp.int32, shape, 0)


def bucket_of(offset):
    distance = jnp.abs(offset)
    bucket = jnp.where(offset > 0, 16, 0)
    for threshold in thresholds:
        bucket = bucket + jnp.where(distance >= threshold, 1, 0)
    return bucket


def bits_of(count):
    return count.bit_length() - 1


def column_parts(width):
    tiles = width // 128
    cuts = [0, (tiles + 2) // 3, (2 * tiles + 2) // 3, tiles]
    return [(cuts[i] * 128, (cuts[i + 1] - cuts[i]) * 128) for i in range(3)]


def flipped(place, bit):
    return place + (1 - 2 * ((place // (1 << bit)) % 2)) * (1 << bit)


class Doubling:
    def __init__(self, at, own, every, sems, core_sems, orders):
        self.at, self.own, self.every = at, own, every
        self.sems, self.core_sems, self.orders = sems, core_sems, orders
        self.plane = at.quad * at.exps + at.exp
        self.steps = len(orders[0])
        self.parts = column_parts(own.shape[1])

    def device(self, bit):
        other = flipped(self.plane, bit)
        return (self.at.grp, other // self.at.exps, other % self.at.exps)

    def place(self, part, j):
        p = self.plane
        for i, bit in enumerate(self.orders[part]):
            if (j >> i) & 1:
                p = flipped(p, bit + 1)
        return p

    def block(self, part, p):
        begin, size = self.parts[part]
        return self.every.at[p, :, pl.ds(begin, size)]

    def source(self, part, j):
        begin, size = self.parts[part]
        return self.own.at[:, pl.ds(begin, size)] if j == 0 else self.block(part, self.place(part, j))

    def index(self, step, part, j):
        return part * (1 << self.steps) + (1 << step) - 1 + j

    def copy(self, step, part, j):
        i = self.index(step, part, j)
        return send(
            self.source(part, j),
            self.block(part, self.place(part, j)),
            self.sems.at[0, i],
            self.sems.at[1, i],
            self.device(self.orders[part][step] + 1),
        )

    def core_copy(self, part, j):
        i = part * (1 << self.steps) + j
        return send(
            self.source(part, j),
            self.block(part, self.place(part, j)),
            self.core_sems.at[0, i],
            self.core_sems.at[1, i],
            self.device(0),
        )

    def start(self):
        for part in range(3):
            for step in range(self.steps):
                self.copy(step, part, 0).start()
        for part in range(3):
            self.core_copy(part, 0).start()
        self.keep().start()

    def keep(self):
        return pltpu.make_async_copy(self.own, self.every.at[self.plane], self.core_sems.at[1, 3 << self.steps])

    def next(self, step):
        for part in range(3):
            for j in range(1 << step):
                k = (1 << step) + j
                arrived(self.block(part, self.place(part, k)), self.sems.at[1, self.index(step, part, j)])
                for later in range(step + 1, self.steps):
                    self.copy(later, part, k).start()
                self.core_copy(part, k).start()

    def finish_in(self):
        for part in range(3):
            for j in range(1 << self.steps):
                there = self.block(part, flipped(self.place(part, j), 0))
                arrived(there, self.core_sems.at[1, part * (1 << self.steps) + j])
        self.keep().wait()

    def finish_out(self):
        for part in range(3):
            for j in range(1 << self.steps):
                self.core_copy(part, j).wait_send()
            for step in range(self.steps):
                for j in range(1 << step):
                    self.copy(step, part, j).wait_send()


class Tiles:
    def __init__(self, units, reps):
        self.units = units
        self.reps = reps
        self.hidden = units * reps
        self.half = self.hidden // 256
        self.wide = (self.half + 1) // 2
        self.count = 3
        self.size = 128 * self.wide // self.count
        self.skip = 128 * (2 * self.wide - self.half)

    def start(self, quad):
        return 128 * (self.half * (quad // 2) + (self.half - self.wide) * (quad % 2))

    def rows(self, tile):
        result = []
        for k in range(QUAD):
            found = None
            for parity in range(2):
                first = self.start(parity) + tile * self.size
                live = first + (self.skip if parity and tile == 0 else 0)
                begin = max(live, k * self.units)
                end = min(first + self.size, (k + 1) * self.units)
                if end > begin:
                    found = (begin - k * self.units, end - begin, parity, begin - first)
            result.append(found)
        return result


class Outward:
    def __init__(self, at, tiles, tile, in_low, down_slab, both_w, down_w, nothing, sems, down_sems):
        self.at, self.tiles, self.tile = at, tiles, tile
        self.in_low, self.down_slab, self.both_w, self.down_w = in_low, down_slab, both_w, down_w
        self.nothing, self.sems, self.down_sems = nothing, sems, down_sems
        self.slab = in_low.shape[0]

    def source(self, quad, section):
        begin = section * self.tiles.hidden + self.tiles.start(quad) + self.tile * self.tiles.size
        return self.in_low.at[:, pl.ds(pl.multiple_of(begin, 128), self.tiles.size)]

    def target(self, rep, section):
        rows = pl.ds(pl.multiple_of(rep * self.slab, self.slab), self.slab)
        return self.both_w.at[rows, pl.ds(section * self.tiles.size, self.tiles.size)]

    def over(self, act):
        at = self.at

        def one(k, _):
            other = (at.rep + k) % at.reps
            for section in range(2):
                act(
                    functools.partial(
                        send,
                        self.source(other % QUAD, section),
                        self.target(at.rep, section),
                        self.sems.at[0, section * at.reps + other],
                        self.sems.at[1, section * at.reps + at.rep],
                        at.device(other, at.exp),
                    )
                )
            return 0

        lax.fori_loop(1, at.reps, one, 0)

    def over_down(self, act, act_local):
        at = self.at
        for k, piece in enumerate(self.tiles.rows(self.tile)):
            if piece is None:
                continue
            begin, count, parity, to = piece
            quad = 2 * (at.rep // QUAD) + parity
            src, dst = self.down_slab.at[pl.ds(begin, count)], self.down_w.at[pl.ds(to, count)]
            recv = self.down_sems.at[1, at.rep]
            for g in range(at.grps):
                stays = jnp.logical_and(at.grp == g, at.quad == quad)
                ours = at.rep % QUAD == k

                @pl.when(jnp.logical_and(ours, jnp.logical_not(stays)))
                def _():
                    act(functools.partial(send, src, dst, self.down_sems.at[0, g], recv, (g, quad, at.exp)))

                @pl.when(jnp.logical_and(ours, stays))
                def _():
                    act_local(functools.partial(pltpu.make_async_copy, src, dst, recv))

    def blank(self):
        return pltpu.make_async_copy(
            self.nothing, self.down_w.at[pl.ds(0, self.tiles.skip)], self.down_sems.at[1, self.at.reps]
        )

    def start(self):
        at = self.at
        self.over_down(lambda copy: copy().start(), lambda copy: copy().start())
        self.over(lambda copy: copy().start())
        for section in range(2):
            pltpu.make_async_copy(
                self.source(at.quad, section), self.target(at.rep, section), self.sems.at[1, section * at.reps + at.rep]
            ).start()
        if self.tile == 0:

            @pl.when(at.quad % 2 == 1)
            def _():
                self.blank().start()

    def arrive(self):
        at = self.at

        def one(rep, _):
            for section in range(2):
                arrived(self.target(rep, section), self.sems.at[1, section * at.reps + rep])
            return 0

        lax.fori_loop(0, at.reps, one, 0)
        for parity in range(2):

            @pl.when(at.quad % 2 == parity)
            def _():
                for k, piece in enumerate(self.tiles.rows(self.tile)):
                    if piece is not None and piece[2] == parity:
                        source = QUAD * (at.quad // 2) + k
                        arrived(self.down_w.at[pl.ds(piece[3], piece[1])], self.down_sems.at[1, source])
                if parity and self.tile == 0:
                    self.blank().wait()

    def sent(self):
        self.over(lambda copy: copy().wait_send())
        self.over_down(lambda copy: copy().wait_send(), lambda copy: None)


class Homeward:
    def __init__(self, at, tiles, tile, both, down, in_parts, down_parts, sems, down_sems):
        self.at, self.tiles, self.tile = at, tiles, tile
        self.both, self.down, self.in_parts, self.down_parts = both, down, in_parts, down_parts
        self.sems, self.down_sems = sems, down_sems
        self.slab = in_parts.shape[1]

    def target(self, grp, quad, parity, section):
        skip = self.tiles.skip if parity and self.tile == 0 else 0
        to = section * self.tiles.hidden + self.tiles.start(quad) + self.tile * self.tiles.size + skip
        to = to if isinstance(to, int) else pl.multiple_of(to, 128)
        return skip, self.in_parts.at[grp, :, pl.ds(to, self.tiles.size - skip)]

    def copy(self, rep, parity, section, local=False):
        at = self.at
        skip, dst = self.target(at.grp, at.quad, parity, section)
        rows = pl.ds(pl.multiple_of(rep * self.slab, self.slab), self.slab)
        src = self.both.at[rows, pl.ds(section * self.tiles.size + skip, self.tiles.size - skip)]
        recv = self.sems.at[1, section * at.reps + at.rep]
        if local:
            return pltpu.make_async_copy(src, dst, recv)
        return send(src, dst, self.sems.at[0, section * at.reps + rep], recv, at.device(rep, at.exp))

    def over(self, act, act_local):
        at = self.at
        for parity in range(2):

            @pl.when(at.quad % 2 == parity)
            def _():
                def one(k, _):
                    for section in range(2):
                        act(self.copy((at.rep + k) % at.reps, parity, section))
                    return 0

                lax.fori_loop(1, at.reps, one, 0)
                if act_local:
                    for section in range(2):
                        act_local(self.copy(at.rep, parity, section, local=True))

    def over_down(self, act, act_local):
        at = self.at
        for k, piece in enumerate(self.tiles.rows(self.tile)):
            if piece is None:
                continue
            begin, count, parity, to = piece
            src, dst = self.down.at[pl.ds(to, count)], self.down_parts.at[at.grp, pl.ds(begin, count)]
            recv = self.down_sems.at[1, at.grp]
            stays = jnp.logical_and(at.grp == at.quad // 2, at.quad == k)
            ours = at.quad % 2 == parity

            @pl.when(jnp.logical_and(ours, jnp.logical_not(stays)))
            def _():
                act(functools.partial(send, src, dst, self.down_sems.at[0, k], recv, (at.quad // 2, k, at.exp)))

            @pl.when(jnp.logical_and(ours, stays))
            def _():
                act_local(functools.partial(pltpu.make_async_copy, src, dst, recv))

    def start(self):
        self.over_down(lambda copy: copy().start(), lambda copy: copy().start())
        self.over(lambda copy: copy.start(), lambda copy: copy.start())

    def arrive(self):
        at = self.at
        for rep in range(at.reps):
            for section in range(2):
                _, dst = self.target(rep // QUAD, rep % QUAD, rep % 2, section)
                arrived(dst, self.sems.at[1, section * at.reps + rep])
        for k, piece in enumerate(self.tiles.rows(self.tile)):
            if piece is None:
                continue

            @pl.when(at.quad == k)
            def _():
                for g in range(at.grps):
                    arrived(self.down_parts.at[g, pl.ds(piece[0], piece[1])], self.down_sems.at[1, g])

    def sent(self):
        self.over(lambda copy: copy.wait_send(), None)
        self.over_down(lambda copy: copy().wait_send(), lambda copy: None)


def forward_kernel(
    grps,
    exps,
    lengths,
    bias_table,
    routes_t,
    tokens,
    cotangent,
    gains,
    router,
    qkv_t,
    out_w,
    in_low,
    down_slab,
    both_w,
    down_w,
    cot_all,
    n_all,
    comb_all,
    qkv_out,
    lse_out,
    mine_out,
    n1_out,
    wqkv_out,
    wout_out,
    h1_out,
    n2_out,
    probs_out,
    tok_all,
    wqkv,
    wout,
    n1,
    qkv,
    lse,
    mine,
    ctx,
    bias,
    comb_send,
    nothing,
    tok_sem,
    wq_sem,
    pass_sem,
    wo_sem,
    wo2_sem,
    weight_sem,
    down_sem,
    ctx_sem,
    cot_sem,
    cot_core_sem,
    n_sem,
    n_core_sem,
    comb_sem,
    store_sem,
):
    at = Where(grps, exps)
    reps = at.reps
    rows, width = tokens.shape
    heads = HEADS // exps
    head_dim = width // HEADS
    head_cols = heads * head_dim
    block_cols = min(128, head_cols)
    shard_cols, row_block = qkv_t.shape
    seg = math.gcd(shard_cols, head_cols)
    segs = shard_cols // seg
    tiles = Tiles(down_slab.shape[0], reps)
    plane = at.quad * exps + at.exp
    members = QUAD * exps
    scale = 1.0 / math.sqrt(head_dim)
    SEND, RECV = 0, 1

    greet_all(at)

    def exp_peer(k):
        return (at.exp + k) % exps

    for k in range(1, exps):
        peer = exp_peer(k)
        send(
            tokens, tok_all.at[at.exp], tok_sem.at[SEND, peer], tok_sem.at[RECV, at.exp], at.device(at.rep, peer)
        ).start()
    tok_all[at.exp] = tokens[...]

    def segment(k):
        col = (at.rep * segs + k) * seg
        section = col // width
        within = col - section * width
        owner = within // head_cols
        return owner, section * head_cols + within - owner * head_cols

    seg_count = 3 * head_cols // seg

    def segment_copy(k, shift):
        owner, offset = segment(k)
        src = qkv_t.at[pl.ds(k * seg, seg)]
        dst = wqkv.at[at.exp, pl.ds(pl.multiple_of(offset, seg), seg)]
        grp = jnp.where(shift < QUAD, at.grp, (at.grp + shift - QUAD + 1) % grps)
        quad = jnp.where(shift < QUAD, (at.quad + shift) % QUAD, at.quad)
        return owner, src, dst, functools.partial(
            send,
            src,
            dst,
            wq_sem.at[SEND, k * fan + shift],
            wq_sem.at[RECV, at.exp * seg_count + offset // seg],
            (grp, quad, owner),
        )

    fan = QUAD + grps - 1

    def over_segments(act, act_local):
        def one(i, _):
            k, shift = i // fan, i % fan
            owner, src, dst, copy = segment_copy(k, shift)
            stays = jnp.logical_and(shift == 0, owner == at.exp)

            @pl.when(jnp.logical_not(stays))
            def _():
                act(copy())

            @pl.when(stays)
            def _():
                act_local(k, src, dst)

            return 0

        lax.fori_loop(0, segs * fan, one, 0)

    def local_segment(k, src, dst):
        _, offset = segment(k)
        pltpu.make_async_copy(src, dst, wq_sem.at[RECV, at.exp * seg_count + offset // seg]).start()

    over_segments(lambda copy: copy.start(), local_segment)

    def over_passed(act):
        def one(i, _):
            e, j = i // seg_count, i % seg_count
            col = (j // (head_cols // seg)) * width + at.exp * head_cols + (j % (head_cols // seg)) * seg
            rep = col // seg // segs

            @pl.when(jnp.logical_and(rep % QUAD == at.quad, rep != at.rep))
            def _():
                block = wqkv.at[e, pl.ds(pl.multiple_of(j * seg, seg), seg)]
                act(i, block)

            return 0

        lax.fori_loop(0, exps * seg_count, one, 0)

    def passed_copies(i, block):
        return [
            send(
                block,
                block,
                pass_sem.at[i, k - 1],
                wq_sem.at[RECV, i],
                (at.grp, (at.quad + k) % QUAD, at.exp),
            )
            for k in range(1, QUAD)
        ]

    def pass_on(i, block):
        arrived(block, wq_sem.at[RECV, i])
        for copy in passed_copies(i, block):
            copy.start()

    def passed_sent(i, block):
        for copy in passed_copies(i, block):
            copy.wait_send()

    for k in range(1, reps):
        other = (at.rep + k) % reps
        send(
            out_w, wout.at[at.exp, at.rep], wo_sem.at[SEND, other], wo_sem.at[RECV, at.rep], at.device(other, at.exp)
        ).start()
    wout[at.exp, at.rep] = out_w[...]
    chip_bits = list(range(bits_of(members) - 1))
    cots = Doubling(at, cotangent, cot_all, cot_sem, cot_core_sem, [chip_bits[::-1]] * 3)
    cots.start()

    span = 2 * rows
    bucket = bucket_of(lane_of((8, span)) - rows)
    for h in range(heads):
        line = jnp.zeros((8, span), full)
        for b in range(BUCKETS):
            line = jnp.where(bucket == b, bias_table[at.exp * heads + h, b], line)
        whole = jnp.broadcast_to(line[0:1], (rows, span))
        bias[h] = pltpu.roll(whole, 0, 1, stride=1, stride_axis=0)[:, rows:]

    over_passed(pass_on)

    def norm_group(s, _):
        @pl.when(s != at.exp)
        def _():
            arrived(tok_all.at[s], tok_sem.at[RECV, s])

        x = tok_all[s].astype(full)
        r = lax.rsqrt(jnp.mean(x * x, axis=1, keepdims=True) + eps_norm)
        n1[s] = (x * r * gains[0:1, :]).astype(low)
        return 0

    lax.fori_loop(0, exps, norm_group, 0)

    nothing[...] = jnp.zeros_like(nothing)
    weights = [
        Outward(
            at, tiles, t, in_low, down_slab, both_w.at[t], down_w.at[t], nothing, weight_sem.at[t], down_sem.at[t]
        )
        for t in range(2)
    ]
    weights[0].start()

    def wait_segment(i, _):
        e, j = i // seg_count, i % seg_count
        col = (j // (head_cols // seg)) * width + at.exp * head_cols + (j % (head_cols // seg)) * seg
        rep = col // seg // segs

        @pl.when(jnp.logical_not(jnp.logical_and(rep % QUAD == at.quad, rep != at.rep)))
        def _():
            arrived(wqkv.at[e, pl.ds(pl.multiple_of(j * seg, seg), seg)], wq_sem.at[RECV, i])

        return 0

    lax.fori_loop(0, exps * seg_count, wait_segment, 0)

    def project(s, _):
        total = jnp.zeros((rows, 3 * head_cols), full)
        for e in range(exps):
            total = total + nt(n1[s, :, e * row_block : (e + 1) * row_block], wqkv[e])
        qkv[s] = total.astype(low)
        return 0

    lax.fori_loop(0, exps, project, 0)

    for k in range(1, reps):
        other = (at.rep + k) % reps
        arrived(wout.at[at.exp, other], wo_sem.at[RECV, other])

    def wout_copies():
        return [
            send(
                wout.at[at.exp],
                wout.at[at.exp],
                wo2_sem.at[SEND, exp_peer(k)],
                wo2_sem.at[RECV, at.exp],
                at.device(at.rep, exp_peer(k)),
            )
            for k in range(1, exps)
        ]

    for copy in wout_copies():
        copy.start()

    cots.next(0)

    def attend(i, _):
        s = (at.exp + 1 + i) % exps
        ok = lane_of((rows, rows)) < lengths[at.base + s]
        lane = lane_of((rows, block_cols))
        sums = jnp.zeros((rows, 128), full)
        for c in range(head_cols // block_cols):
            cols = slice(c * block_cols, (c + 1) * block_cols)
            q = qkv[s, :, cols]
            k = qkv[s, :, head_cols + c * block_cols : head_cols + (c + 1) * block_cols]
            v = qkv[s, :, 2 * head_cols + c * block_cols : 2 * head_cols + (c + 1) * block_cols]
            result = jnp.zeros((rows, block_cols), full)
            for t in range(block_cols // head_dim):
                h = c * (block_cols // head_dim) + t
                here = jnp.logical_and(lane >= t * head_dim, lane < (t + 1) * head_dim)
                scores = nt(jnp.where(here, q, jnp.zeros_like(q)), k) * scale + bias[h]
                scores = jnp.where(ok, scores, -1e30)
                top = jnp.max(scores, axis=1, keepdims=True)
                weights = jnp.exp(scores - top)
                total = jnp.sum(weights, axis=1, keepdims=True)
                weights = (weights * (1.0 / total)).astype(low)
                result = jnp.where(here, jnp.dot(weights, v, preferred_element_type=full), result)
                sums = jnp.where(lane_of((rows, 128)) == h, top + jnp.log(total), sums)
            mine[s, :, cols] = result.astype(low)
        lse[s] = sums

        @pl.when(i < exps - 1)
        def _():
            send(
                mine.at[s], ctx.at[at.exp], ctx_sem.at[SEND, s], ctx_sem.at[RECV, at.exp], at.device(at.rep, s)
            ).start()

        @pl.when(i == exps - 1)
        def _():
            pltpu.make_async_copy(mine.at[s], ctx.at[at.exp], ctx_sem.at[RECV, at.exp]).start()

        return 0

    lax.fori_loop(0, exps, attend, 0)

    cots.next(1)
    for k in range(1, exps):
        arrived(wout.at[exp_peer(k)], wo2_sem.at[RECV, exp_peer(k)])
    for e in range(exps):
        arrived(ctx.at[e], ctx_sem.at[RECV, e])

    out_cols = wout.shape[3]
    for r in range(reps):
        cols = slice(r * out_cols, (r + 1) * out_cols)
        total = tokens[:, cols].astype(full)
        for e in range(exps):
            total = total + jnp.dot(ctx[e], wout[e, r], preferred_element_type=full)
        h1_out[:, cols] = total
    h1 = h1_out[...]
    r2 = lax.rsqrt(jnp.mean(h1 * h1, axis=1, keepdims=True) + eps_norm)
    n2 = (h1 * r2 * gains[1:2, :]).astype(low)
    n2_out[...] = n2
    rotated = [chip_bits[c:] + chip_bits[:c] for c in range(3)]
    rows_two = Doubling(at, n2_out, n_all, n_sem, n_core_sem, rotated)
    rows_two.start()
    weights[1].start()

    router_rows = jnp.concatenate([router[...], jnp.zeros((128 - exps, width), full)], axis=0)
    logits = nt(n2.astype(full), router_rows, precision=highest)
    lane = lane_of((rows, 128))
    logits = jnp.where(lane < exps, logits, -1e30)
    probs = jnp.exp(logits - jnp.max(logits, axis=1, keepdims=True))
    probs = probs / jnp.sum(probs, axis=1, keepdims=True)
    probs_out[...] = probs
    picked = jnp.where(routed(routes_t, at.me, rows), probs, 0.0)
    comb = picked / jnp.sum(picked, axis=1, keepdims=True)
    comb = jnp.where(row_of((rows, 1)) < lengths[at.me], comb, 0.0)
    comb_send[...] = comb.T[0 : comb_send.shape[0]]

    def comb_copy(k):
        other = (plane + k) % members
        return send(
            comb_send,
            comb_all.at[plane],
            comb_sem.at[SEND, other],
            comb_sem.at[RECV, plane],
            (at.grp, other // exps, other % exps),
        )

    def start_comb(k, _):
        comb_copy(k).start()
        return 0

    lax.fori_loop(1, members, start_comb, 0)
    pltpu.make_async_copy(comb_send, comb_all.at[plane], comb_sem.at[RECV, plane]).start()
    rows_two.next(0)

    stores = [
        (qkv, qkv_out),
        (lse, lse_out),
        (mine, mine_out),
        (n1, n1_out),
        (wqkv, wqkv_out),
        (wout, wout_out),
    ]
    for i, (src, dst) in enumerate(stores):
        pltpu.make_async_copy(src, dst, store_sem.at[i]).start()

    for step in range(1, rows_two.steps):
        rows_two.next(step)
    for step in range(2, cots.steps):
        cots.next(step)

    cots.finish_in()
    rows_two.finish_in()

    def comb_in(k, _):
        arrived(comb_all.at[k], comb_sem.at[RECV, k])
        return 0

    lax.fori_loop(0, members, comb_in, 0)
    for tile in weights:
        tile.arrive()

    for k in range(1, exps):
        peer = exp_peer(k)
        arrived(tokens, tok_sem.at[SEND, peer])
        arrived(mine.at[peer], ctx_sem.at[SEND, peer])
    over_segments(lambda copy: copy.wait_send(), lambda k, src, dst: None)
    over_passed(passed_sent)
    for k in range(1, reps):
        arrived(out_w, wo_sem.at[SEND, (at.rep + k) % reps])
    for copy in wout_copies():
        copy.wait_send()
    cots.finish_out()
    rows_two.finish_out()

    def sent_comb(k, _):
        comb_copy(k).wait_send()
        return 0

    lax.fori_loop(1, members, sent_comb, 0)
    for tile in weights:
        tile.sent()
    for i, (src, dst) in enumerate(stores):
        pltpu.make_async_copy(src, dst, store_sem.at[i]).wait()


def forward_call(
    grps, exps, lengths, bias_table, routes_t, tokens, cotangent, gains, router, qkv_t, out_w, in_low, down_slab
):
    reps = grps * QUAD
    rows, width = tokens.shape
    head_cols = width // exps
    row_block = qkv_t.shape[1]
    seg = math.gcd(qkv_t.shape[0], head_cols)
    segs = qkv_t.shape[0] // seg
    units = down_slab.shape[0]
    out_cols = out_w.shape[1]
    heads = HEADS // exps
    members = QUAD * exps
    tiles = Tiles(units, reps)
    shape = jax.ShapeDtypeStruct
    vmem = pl.BlockSpec(memory_space=pltpu.VMEM)
    smem = pl.BlockSpec(memory_space=pltpu.SMEM)
    hbm = pl.BlockSpec(memory_space=pl.ANY)
    results = [
        (shape((2, width, 2 * tiles.size), low), hbm),
        (shape((2, tiles.size, width), low), hbm),
        (shape((members, rows, width), low), hbm),
        (shape((members, rows, width), low), hbm),
        (shape((members, 8, rows), full), hbm),
        (shape((exps, rows, 3 * head_cols), low), hbm),
        (shape((exps, rows, 128), full), hbm),
        (shape((exps, rows, head_cols), low), hbm),
        (shape((exps, rows, width), low), hbm),
        (shape((exps, 3 * head_cols, row_block), low), hbm),
        (shape((exps, reps, row_block, out_cols), low), hbm),
        (shape((rows, width), full), vmem),
        (shape((rows, width), low), vmem),
        (shape((rows, 128), full), vmem),
    ]
    dma = pltpu.SemaphoreType.DMA
    chips = members // 2
    return pl.pallas_call(
        functools.partial(forward_kernel, grps, exps),
        out_shape=[r[0] for r in results],
        in_specs=[smem] * 2 + [vmem] * 7 + [hbm] * 2,
        out_specs=[r[1] for r in results],
        scratch_shapes=[
            pltpu.VMEM((exps, rows, width), low),
            pltpu.VMEM((exps, 3 * head_cols, row_block), low),
            pltpu.VMEM((exps, reps, row_block, out_cols), low),
            pltpu.VMEM((exps, rows, width), low),
            pltpu.VMEM((exps, rows, 3 * head_cols), low),
            pltpu.VMEM((exps, rows, 128), full),
            pltpu.VMEM((exps, rows, head_cols), low),
            pltpu.VMEM((exps, rows, head_cols), low),
            pltpu.VMEM((heads, rows, rows), full),
            pltpu.VMEM((8, rows), full),
            pltpu.VMEM((tiles.skip, width), low),
            dma((2, exps)),
            dma((2, max(segs * (QUAD + grps - 1), exps * 3 * head_cols // seg))),
            dma((exps * 3 * head_cols // seg, QUAD - 1)),
            dma((2, reps)),
            dma((2, exps)),
            dma((2, 2, 2 * reps)),
            dma((2, 2, reps + 1)),
            dma((2, exps)),
            dma((2, 3 * chips)),
            dma((2, 3 * chips + 1)),
            dma((2, 3 * chips)),
            dma((2, 3 * chips + 1)),
            dma((2, members)),
            dma((6,)),
        ],
        compiler_params=pltpu.CompilerParams(
            collective_id=0, has_side_effects=True, vmem_limit_bytes=60 * 1024 * 1024
        ),
        name="forward",
    )(lengths, bias_table, routes_t, tokens, cotangent, gains, router, qkv_t, out_w, in_low, down_slab)


def expert_kernel(
    grps,
    exps,
    cap,
    deal,
    routes_t,
    comb,
    n_all,
    cot_all,
    both_w,
    down_w,
    in_low,
    down_slab,
    n_sum,
    y_sum,
    c_sum,
    both_g,
    down_g,
    in_parts,
    down_parts,
    place,
    marks,
    n_rows,
    g_rows,
    both_v,
    down_v,
    raw_n,
    raw_g,
    y_acc,
    n_acc,
    both_d,
    active,
    both_stage,
    down_stage,
    out_n,
    out_y,
    load_sem,
    raw_sem,
    out_sem,
    in_sem,
    in_down_sem,
    home_sem,
    home_down_sem,
    stage_sem,
):
    at = Where(grps, exps)
    rows, width = n_all.shape[1:]
    tiles = Tiles(down_slab.shape[0], at.reps)
    size = tiles.size
    slots = exps * cap
    members = QUAD * exps
    loads = [pltpu.make_async_copy(both_w.at[t], both_v.at[t], load_sem.at[0, t]) for t in range(2)] + [
        pltpu.make_async_copy(down_w.at[t], down_v.at[t], load_sem.at[1, t]) for t in range(2)
    ]
    for copy in loads:
        copy.start()

    def raw_copies(q):
        here = pl.ds(pl.multiple_of(q * exps, exps), exps)
        return [
            pltpu.make_async_copy(n_all.at[here], raw_n.at[q % 2], raw_sem.at[0, q % 2]),
            pltpu.make_async_copy(cot_all.at[here], raw_g.at[q % 2], raw_sem.at[1, q % 2]),
        ]

    for copy in raw_copies(0):
        copy.start()
    greet_all(at)
    last = tiles.count - 1
    incoming = Outward(
        at, tiles, last, in_low, down_slab, both_v.at[last], down_v.at[last], None, in_sem, in_down_sem
    )
    incoming.start()
    home = Homeward(
        at, tiles, 0, both_stage.at[0], down_stage.at[0], in_parts, down_parts, home_sem, home_down_sem
    )

    earlier = jnp.where(row_of((rows, rows)) < lane_of((rows, rows)), 1.0, 0.0).astype(low)
    slot = row_of((cap, rows)).astype(full)

    def dispatch(q, _):
        @pl.when(q + 1 < QUAD)
        def _():
            for copy in raw_copies(q + 1):
                copy.start()

        for copy in raw_copies(q):
            copy.wait()
        lines = []
        for j in range(exps):
            seq = at.grp * members + q * exps + j
            pair = routes_t[:, pl.ds(pl.multiple_of(seq * rows, rows), rows)]
            lines.append(jnp.logical_or(pair[0:1] == at.exp, pair[1:2] == at.exp))
        lines = [jnp.where(line, 1.0, 0.0) for line in lines] + [jnp.zeros((8 - exps, rows), full)]
        hot_low = jnp.concatenate(lines, axis=0).astype(low)
        before = dot(hot_low, earlier)
        for j in range(exps):
            s = q * exps + j
            inside = jnp.logical_and(slot == before[j : j + 1, :], hot_low[j : j + 1, :].astype(full) > 0.5)
            here = jnp.where(inside, 1.0, 0.0)
            place[s] = here.astype(low)
            g = raw_g[q % 2, 0]
            for b in range(1, exps):
                g = jnp.where(deal[at.grp * members + s] == at.grp * members + q * exps + b, raw_g[q % 2, b], g)
            where = pl.ds(pl.multiple_of(s * cap, cap), cap)
            n_rows[where] = dot(here.astype(low), raw_n[q % 2, j]).astype(low)
            g_rows[where] = dot(here.astype(low), g).astype(low)
            marks[where, 0:1] = jnp.sum(here * comb[s, pl.ds(at.exp, 1), :], axis=1, keepdims=True)
            marks[where, 1:2] = jnp.zeros((cap, 1), full)
        return 0

    lax.fori_loop(0, QUAD, dispatch, 0)
    for copy in loads:
        copy.wait()
    curve = math.sqrt(2.0 / math.pi)

    def tile_work(f, _):
        @pl.when(f == last)
        def _():
            incoming.arrive()

        def chunk(c, _):
            here = pl.ds(pl.multiple_of(c * slots, slots), slots)
            share = marks[here, 0:1]
            both = dot(n_rows[here], both_v[f])
            gate_part, up_part = both[:, :size], both[:, size:]
            grad = nt(g_rows[here], down_v[f])
            square = gate_part * gate_part
            bend = jnp.tanh(curve * gate_part * (1.0 + 0.044715 * square))
            half = 0.5 * (1.0 + bend)
            gelu = gate_part * half
            slope = half + (0.5 * curve) * gate_part * (1.0 - bend * bend) * (1.0 + (3 * 0.044715) * square)
            value = gelu * up_part
            marks[here, 1:2] += jnp.sum(value * grad, axis=1, keepdims=True)
            grad = grad * share
            active[here] = (value * share).astype(low)
            both_d[here, :size] = (grad * up_part * slope).astype(low)
            both_d[here, size:] = (grad * gelu).astype(low)
            y = dot(active[here], down_v[f])
            y_acc[here] = jnp.where(f == 0, y, y_acc[here].astype(full) + y).astype(low)
            n_back = nt(both_d[here], both_v[f])
            n_acc[here] = jnp.where(f == 0, n_back, n_acc[here] + n_back)
            return 0

        lax.fori_loop(0, QUAD, chunk, 0)

        def columns(m, _):
            cols = pl.ds(pl.multiple_of(m * (width // 2), width // 2), width // 2)
            both_stage[f, cols] = tn(n_rows[:, cols], both_d[...]).astype(low)
            down_stage[f, :, cols] = tn(active[...], g_rows[:, cols]).astype(low)
            return 0

        lax.fori_loop(0, 2, columns, 0)

        @pl.when(f == 0)
        def _():
            home.start()

        @pl.when(f > 0)
        def _():
            for copy in stage_copies(f):
                copy.start()

        return 0

    def stage_copies(f):
        return [
            pltpu.make_async_copy(both_stage.at[f], both_g.at[f - 1], stage_sem.at[0, f]),
            pltpu.make_async_copy(down_stage.at[f], down_g.at[f - 1], stage_sem.at[1, f]),
        ]

    lax.fori_loop(0, tiles.count, tile_work, 0)

    def out_copies(s):
        return [
            pltpu.make_async_copy(out_n.at[s % 2], n_sum.at[s], out_sem.at[0, s % 2]),
            pltpu.make_async_copy(out_y.at[s % 2], y_sum.at[s], out_sem.at[1, s % 2]),
        ]

    def gather(s, _):
        @pl.when(s >= 2)
        def _():
            for copy in out_copies(s - 2):
                copy.wait()

        where = pl.ds(pl.multiple_of(s * cap, cap), cap)
        out_n[s % 2] = tn(place[s], n_acc[where].astype(low)).astype(low)
        out_y[s % 2] = tn(place[s], y_acc[where]).astype(low)
        line = jnp.sum(place[s].astype(full) * marks[where, 1:2], axis=0, keepdims=True)
        c_sum[s] = jnp.broadcast_to(line, (8, rows))
        for copy in out_copies(s):
            copy.start()
        return 0

    lax.fori_loop(0, members, gather, 0)
    for s in (members - 2, members - 1):
        for copy in out_copies(s):
            copy.wait()
    for f in range(1, tiles.count):
        for copy in stage_copies(f):
            copy.wait()
    home.arrive()
    incoming.sent()
    home.sent()


def expert_call(grps, exps, cap, deal, routes_t, comb_all, n_all, cot_all, both_w, down_w, in_low, down_slab):
    members, rows, width = n_all.shape
    reps = grps * QUAD
    tiles = Tiles(down_slab.shape[0], reps)
    size = tiles.size
    slab, both_hidden = in_low.shape
    units = down_slab.shape[0]
    slots = exps * cap
    shape = jax.ShapeDtypeStruct
    vmem = pl.BlockSpec(memory_space=pltpu.VMEM)
    smem = pl.BlockSpec(memory_space=pltpu.SMEM)
    hbm = pl.BlockSpec(memory_space=pl.ANY)
    results = [
        (shape((members, rows, width), low), hbm),
        (shape((members, rows, width), low), hbm),
        (shape((members, 8, rows), full), vmem),
        (shape((2, width, 2 * size), low), hbm),
        (shape((2, size, width), low), hbm),
        (shape((grps, slab, both_hidden), low), hbm),
        (shape((grps, units, width), low), hbm),
    ]
    dma = pltpu.SemaphoreType.DMA
    return pl.pallas_call(
        functools.partial(expert_kernel, grps, exps, cap),
        out_shape=[r[0] for r in results],
        in_specs=[smem] + [vmem] * 2 + [hbm] * 6,
        out_specs=[r[1] for r in results],
        scratch_shapes=[
            pltpu.VMEM((members, cap, rows), low),
            pltpu.VMEM((QUAD * slots, 128), full),
            pltpu.VMEM((QUAD * slots, width), low),
            pltpu.VMEM((QUAD * slots, width), low),
            pltpu.VMEM((tiles.count, width, 2 * size), low),
            pltpu.VMEM((tiles.count, size, width), low),
            pltpu.VMEM((2, exps, rows, width), low),
            pltpu.VMEM((2, exps, rows, width), low),
            pltpu.VMEM((QUAD * slots, width), low),
            pltpu.VMEM((QUAD * slots, width), full),
            pltpu.VMEM((QUAD * slots, 2 * size), low),
            pltpu.VMEM((QUAD * slots, size), low),
            pltpu.VMEM((tiles.count, width, 2 * size), low),
            pltpu.VMEM((tiles.count, size, width), low),
            pltpu.VMEM((2, rows, width), low),
            pltpu.VMEM((2, rows, width), low),
            dma((2, 2)),
            dma((2, 2)),
            dma((2, 2)),
            dma((2, 2 * reps)),
            dma((2, reps + 1)),
            dma((2, 2 * reps)),
            dma((2, max(QUAD, grps))),
            dma((2, tiles.count)),
        ],
        compiler_params=pltpu.CompilerParams(
            collective_id=2, has_side_effects=True, vmem_limit_bytes=60 * 1024 * 1024
        ),
        name="experts",
    )(deal, routes_t, comb_all, n_all, cot_all, both_w, down_w, in_low, down_slab)


class Halving:
    def __init__(self, at, source, kept, bufs, sems, load_sem):
        self.at, self.source, self.kept, self.bufs = at, source, kept, bufs
        self.sems, self.load_sem = sems, load_sem
        self.plane = at.quad * at.exps + at.exp
        self.places = bits_of(QUAD * at.exps)
        self.chip_bits = list(range(self.places - 1))
        self.parts = column_parts(source.shape[2])
        self.orders = [self.chip_bits[c:] + self.chip_bits[:c] for c in range(3)]

    def device(self, bit):
        other = flipped(self.plane, bit)
        return (self.at.grp, other // self.at.exps, other % self.at.exps)

    def first(self):
        core = self.plane % 2
        count = 1 << (self.places - 1)
        device = self.device(0)

        def copies(j):
            return send(
                self.source.at[2 * j + 1 - core], self.bufs[0].at[j], self.sems.at[0, 0, j], self.sems.at[0, 1, j], device
            )

        def load(j):
            return pltpu.make_async_copy(self.source.at[2 * j + core], self.kept.at[j], self.load_sem.at[j])

        return count, copies, load

    def start_first(self):
        count, copies, load = self.first()

        def one(j, _):
            copies(j).start()
            load(j).start()
            return 0

        lax.fori_loop(0, count, one, 0)

    def add_first(self):
        count, copies, load = self.first()

        def one(j, _):
            arrived(self.bufs[0].at[j], self.sems.at[0, 1, j])
            load(j).wait()
            self.bufs[0][j] = (self.bufs[0][j].astype(full) + self.kept[j].astype(full)).astype(low)
            return 0

        lax.fori_loop(0, count, one, 0)

    def hop(self, step, part):
        order = self.orders[part]
        bit = order[step]
        left = [b for b in self.chip_bits if b not in order[:step]]
        pos = left.index(bit)
        half = 1 << (len(left) - 1)
        mine = (self.plane // (1 << (bit + 1))) % 2
        device = self.device(bit + 1)
        begin, size = self.parts[part]
        cols = pl.ds(begin, size)
        base = self.base(step, part)

        def index(j, value):
            return (j >> pos) * (1 << (pos + 1)) + value * (1 << pos) + j % (1 << pos)

        pairs = []
        for j in range(half):
            copy = functools.partial(
                send,
                self.bufs[step].at[index(j, 1 - mine), :, cols],
                self.bufs[step + 1].at[j, :, cols],
                self.sems.at[1, 0, base + j],
                self.sems.at[1, 1, base + j],
                device,
            )
            pairs.append((copy, index(j, mine), j))
        return pairs, begin, size, base

    def base(self, step, part):
        n = len(self.chip_bits)
        return part * (1 << n) + sum(1 << (n - 1 - s) for s in range(step))

    def start(self, step, part=None):
        for p in range(3) if part is None else [part]:
            for copy, _, _ in self.hop(step, p)[0]:
                copy().start()

    def add(self, step, part):
        pairs, begin, size, base = self.hop(step, part)
        cols = pl.ds(begin, size)
        here, there = self.bufs[step], self.bufs[step + 1]
        for _, keep, j in pairs:
            arrived(there.at[j, :, cols], self.sems.at[1, 1, base + j])
            there[j, :, begin : begin + size] = (
                there[j, :, begin : begin + size].astype(full) + here[keep, :, begin : begin + size].astype(full)
            ).astype(low)

    def next(self, step):
        for p in range(3):
            self.add(step, p)
            if step + 1 < len(self.chip_bits):
                self.start(step + 1, p)

    def result(self):
        return self.bufs[len(self.chip_bits)]

    def finish(self):
        count, copies, _ = self.first()

        def one(j, _):
            copies(j).wait_send()
            return 0

        lax.fori_loop(0, count, one, 0)
        for step in range(len(self.chip_bits)):
            for p in range(3):
                for copy, _, _ in self.hop(step, p)[0]:
                    copy().wait_send()


def backward_kernel(
    grps,
    exps,
    lengths,
    deal,
    bias_table,
    n_parts,
    y_parts,
    c_parts,
    both_g,
    down_g,
    in_before,
    down_before,
    n1_in,
    cot_all,
    routes_t,
    tokens,
    h1_in,
    n2_in,
    probs_in,
    qkv,
    lse,
    mine,
    wqkv,
    wout,
    *rest,
):
    states, rest = rest[:15], rest[15:]
    token_grad, block_out, in_parts, down_parts = rest[:4]
    news, scratch = rest[4:19], rest[19:]
    (
    kept,
    n_bufs,
    y_bufs,
    c_in,
    dh1,
    dz_send,
    dz_all,
    do_send,
    do_in,
    bias,
    bias_sum,
    dqkv,
    dqkv_t,
    dn1_send,
    dn1_in,
    wq_send,
    og_send,
    qkv_parts,
    out_parts,
    blk_send,
    blk_in,
    small_send,
    small_exp,
    small_sum,
    small_rep,
    bias_grad,
    n_sem,
    y_sem,
    load_sem,
    c_sem,
    weight_sem,
    down_sem,
    dz_sem,
    do_sem,
    dn1_sem,
    wq_sem,
    og_sem,
    blk_sem,
    small_sem,
    small2_sem,
    n1_sem,
    ) = scratch
    at = Where(grps, exps)
    reps = at.reps
    rows, width = tokens.shape
    heads = HEADS // exps
    head_dim = width // HEADS
    head_cols = heads * head_dim
    block_cols = min(128, head_cols)
    row_block = wqkv.shape[2]
    out_cols = wout.shape[3]
    tiles = Tiles(down_parts.shape[1], reps)
    scale = 1.0 / math.sqrt(head_dim)
    SEND, RECV = 0, 1
    plane = at.quad * exps + at.exp
    members = QUAD * exps

    def exp_peer(k):
        return (at.exp + k) % exps

    gains = states[12]
    router = states[9][...]
    n1 = kept.at[0:exps]
    group = pl.ds(pl.multiple_of(at.quad * exps, exps), exps)
    cot_copy = pltpu.make_async_copy(cot_all.at[group], dn1_send, n1_sem.at[1])
    cot_copy.start()
    greet_all(at)

    dn = Halving(at, n_parts, kept, n_bufs, n_sem, load_sem.at[0])
    ys = Halving(at, y_parts, kept, y_bufs, y_sem, load_sem.at[1])
    dn.start_first()
    homes = [
        Homeward(
            at, tiles, t + 1, both_g.at[t], down_g.at[t], in_parts, down_parts, weight_sem.at[t], down_sem.at[t]
        )
        for t in range(2)
    ]
    homes[0].start()
    n1_copy = pltpu.make_async_copy(n1_in, n1, n1_sem.at[0])

    def c_copy(k):
        other = (plane + k) % members
        return other, send(
            c_parts.at[other],
            c_in.at[plane],
            c_sem.at[SEND, other],
            c_sem.at[RECV, plane],
            (at.grp, other // exps, other % exps),
        )

    def start_c(k, _):
        c_copy(k)[1].start()
        return 0

    lax.fori_loop(1, members, start_c, 0)
    pltpu.make_async_copy(c_parts.at[plane], c_in.at[plane], c_sem.at[RECV, plane]).start()

    span = 2 * rows
    bucket = bucket_of(lane_of((8, span)) - rows)
    for h in range(heads):
        line = jnp.zeros((8, span), full)
        for b in range(BUCKETS):
            line = jnp.where(bucket == b, bias_table[at.exp * heads + h, b], line)
        whole = jnp.broadcast_to(line[0:1], (rows, span))
        bias[h] = pltpu.roll(whole, 0, 1, stride=1, stride_axis=0)[:, rows:]

    dn.add_first()
    dn.start(0)
    ys.start_first()

    def wait_c(k, _):
        arrived(c_in.at[k], c_sem.at[RECV, k])
        return 0

    lax.fori_loop(0, members, wait_c, 0)
    lane = lane_of((rows, 128))
    comb_rows = []
    for e in range(exps):
        total = c_in[e]
        for q in range(1, QUAD):
            total = total + c_in[q * exps + e]
        comb_rows.append(total[0:1, :])
    comb_rows.append(jnp.zeros((128 - exps, rows), full))
    comb_grad = jnp.concatenate(comb_rows, axis=0).T
    valid = row_of((rows, 1)) < lengths[at.me]
    probs = probs_in[...]
    hot = routed(routes_t, at.me, rows)
    picked = jnp.where(hot, probs, 0.0)
    total = jnp.sum(picked, axis=1, keepdims=True)
    gate = picked / total
    gate_grad_rows = jnp.where(valid, comb_grad, 0.0)
    spread_grad = jnp.sum(gate_grad_rows * gate, axis=1, keepdims=True)
    probs_grad = jnp.where(hot, (gate_grad_rows - spread_grad) / total, 0.0)
    logit_grad = probs * (probs_grad - jnp.sum(probs_grad * probs, axis=1, keepdims=True))
    n2 = n2_in[...].astype(full)
    router_rows = lax.dot_general(
        logit_grad, n2, (((0,), (0,)), ((), ())), preferred_element_type=full, precision=highest
    )
    small_rows = small_send.shape[0]
    small_send[...] = jnp.zeros_like(small_send)
    small_send[0:exps, :] = router_rows[0:exps, :]
    router_back = jnp.dot(
        logit_grad, jnp.concatenate([router, jnp.zeros((128 - exps, width), full)], axis=0),
        precision=highest, preferred_element_type=full,
    )
    h1 = h1_in[...]
    r2 = lax.rsqrt(jnp.mean(h1 * h1, axis=1, keepdims=True) + eps_norm)

    dn.next(0)
    ys.add_first()
    n1_copy.start()
    dn.next(1)
    steps = len(dn.chip_bits)
    for step in range(2, steps):
        dn.next(step)

    n2_grad = router_back + dn.result()[0].astype(full)
    scaled = n2_grad * gains[1:2, :]
    cot_copy.wait()
    dealt = deal[at.me] - at.base
    g = dn1_send[0]
    for e in range(1, exps):
        g = jnp.where(dealt == e, dn1_send[e], g)
    hidden_grad = (
        jnp.where(valid, g.astype(full), 0.0)
        + r2 * scaled
        - h1 * (r2 * r2 * r2) * jnp.mean(scaled * h1, axis=1, keepdims=True)
    )
    dh1[...] = hidden_grad
    small_send[exps + 1 : exps + 2, :] = jnp.sum(n2_grad * h1 * r2, axis=0, keepdims=True)
    branch = hidden_grad.astype(low)
    dz_send[...] = branch
    for e in range(exps):
        total = jnp.zeros((rows, row_block), full)
        for r in range(reps):
            total = total + nt(branch[:, r * out_cols : (r + 1) * out_cols], wout[e, r])
        do_send[e] = total.astype(low)

    def do_copies():
        return [
            send(
                do_send.at[exp_peer(k)],
                do_in.at[at.exp],
                do_sem.at[SEND, exp_peer(k)],
                do_sem.at[RECV, at.exp],
                at.device(at.rep, exp_peer(k)),
            )
            for k in range(1, exps)
        ]

    for copy in do_copies():
        copy.start()
    pltpu.make_async_copy(do_send.at[at.exp], do_in.at[at.exp], do_sem.at[RECV, at.exp]).start()

    def dz_copies():
        return [
            send(
                dz_send,
                dz_all.at[at.exp],
                dz_sem.at[SEND, exp_peer(k)],
                dz_sem.at[RECV, at.exp],
                at.device(at.rep, exp_peer(k)),
            )
            for k in range(1, exps)
        ]

    for copy in dz_copies():
        copy.start()
    dz_all[at.exp] = branch
    homes[1].start()
    ys.start(0)

    bias_sum[...] = jnp.zeros_like(bias_sum)

    def og_copies():
        return [
            send(
                og_send.at[(at.rep + k) % reps],
                out_parts.at[at.rep],
                og_sem.at[SEND, (at.rep + k) % reps],
                og_sem.at[RECV, at.rep],
                at.device((at.rep + k) % reps, at.exp),
            )
            for k in range(1, reps)
        ]

    def blk_copies():
        return [
            send(
                blk_send,
                blk_in.at[at.exp],
                blk_sem.at[SEND, exp_peer(k)],
                blk_sem.at[RECV, at.exp],
                at.device(at.rep, exp_peer(k)),
            )
            for k in range(1, exps)
        ]

    def beside(k):
        if k < exps - 1:
            ys.next(k - 1)
            return
        for step in range(exps - 2, steps):
            ys.next(step)
        block = jnp.where(valid, h1_in[...] + ys.result()[0].astype(full), 0.0).astype(low)
        blk_send[...] = block
        for copy in blk_copies():
            copy.start()
        blk_in[at.exp] = block
        for j in range(1, exps):
            arrived(dz_all.at[exp_peer(j)], dz_sem.at[RECV, exp_peer(j)])
        grad = tn(mine[...].reshape(exps * rows, head_cols), dz_all[...].reshape(exps * rows, width))
        for r in range(reps):
            og_send[r] = grad[:, r * out_cols : (r + 1) * out_cols].astype(low)
        for copy in og_copies():
            copy.start()
        pltpu.make_async_copy(og_send.at[at.rep], out_parts.at[at.rep], og_sem.at[RECV, at.rep]).start()

    def attend_back(i, _):
        s = (at.exp + 1 + i) % exps
        for k in range(1, exps):

            @pl.when(i == k)
            def _():
                beside(k)

        arrived(do_in.at[s], do_sem.at[RECV, s])
        ok = lane_of((rows, rows)) < lengths[at.base + s]
        block_lane = lane_of((rows, block_cols))
        for c in range(head_cols // block_cols):
            cols = slice(c * block_cols, (c + 1) * block_cols)
            k_cols = slice(head_cols + c * block_cols, head_cols + (c + 1) * block_cols)
            v_cols = slice(2 * head_cols + c * block_cols, 2 * head_cols + (c + 1) * block_cols)
            q = qkv[s, :, cols]
            k = qkv[s, :, k_cols]
            v = qkv[s, :, v_cols]
            do = do_in[s, :, cols]
            dq = jnp.zeros((rows, block_cols), full)
            dk = jnp.zeros((rows, block_cols), full)
            dv = jnp.zeros((rows, block_cols), full)
            for t in range(block_cols // head_dim):
                h = c * (block_cols // head_dim) + t
                here = jnp.logical_and(block_lane >= t * head_dim, block_lane < (t + 1) * head_dim)
                zero = jnp.zeros_like(q)
                q_h = jnp.where(here, q, zero)
                do_h = jnp.where(here, do, zero)
                scores = nt(q_h, k) * scale + bias[h]
                total = jnp.sum(jnp.where(lane == h, lse[s], 0.0), axis=1, keepdims=True)
                p = jnp.where(ok, jnp.exp(scores - total), 0.0)
                dp = nt(do_h, v)
                delta = jnp.sum(dp * p, axis=1, keepdims=True)
                ds = (p * (dp - delta)).astype(low)
                bias_sum[h] += ds.astype(full)
                dv = jnp.where(here, tn(p.astype(low), do), dv)
                dq = jnp.where(here, jnp.dot(ds, k, preferred_element_type=full), dq)
                dk = jnp.where(here, tn(ds, q), dk)
            dqkv[:, cols] = (dq * scale).astype(low)
            dqkv[:, k_cols] = (dk * scale).astype(low)
            dqkv[:, v_cols] = dv.astype(low)
        dqkv_t[:, pl.ds(pl.multiple_of(s * rows, rows), rows)] = dqkv[...].T
        for e in range(exps):
            dn1_send[s, :, e * row_block : (e + 1) * row_block] = jnp.dot(
                dqkv[...], wqkv[e], preferred_element_type=full
            ).astype(low)

        @pl.when(i < exps - 1)
        def _():
            send(
                dn1_send.at[s], dn1_in.at[at.exp], dn1_sem.at[SEND, s], dn1_sem.at[RECV, at.exp], at.device(at.rep, s)
            ).start()

        @pl.when(i == exps - 1)
        def _():
            pltpu.make_async_copy(dn1_send.at[s], dn1_in.at[at.exp], dn1_sem.at[RECV, at.exp]).start()

        return 0

    lax.fori_loop(0, exps, attend_back, 0)

    n1_copy.wait()
    seg = wq_send.shape[2]
    segs = qkv_parts.shape[1]
    parts = wq_send.shape[1]
    for e in range(exps):
        part = kept[0:exps, :, e * row_block : (e + 1) * row_block].reshape(exps * rows, row_block)
        total = dot(dqkv_t[...], part)
        for j in range(parts):
            wq_send[e, j] = total[j * seg : (j + 1) * seg].astype(low)

    def owner(j):
        section, within = j // (head_cols // seg), j % (head_cols // seg)
        col = section * width + at.exp * head_cols + within * seg
        block = col // seg
        return block // segs, block % segs

    def wq_copy(i):
        e, j = i // parts, i % parts
        rep, k = owner(j)
        dst = qkv_parts.at[at.rep, k]
        recv = wq_sem.at[RECV, at.rep * segs + k]
        stays = jnp.logical_and(rep == at.rep, e == at.exp)
        return (
            stays,
            functools.partial(send, wq_send.at[e, j], dst, wq_sem.at[SEND, i], recv, at.device(rep, e)),
            functools.partial(pltpu.make_async_copy, wq_send.at[e, j], dst, recv),
        )

    def start_wq(i, _):
        stays, away, local = wq_copy(i)

        @pl.when(stays)
        def _():
            local().start()

        @pl.when(jnp.logical_not(stays))
        def _():
            away().start()

        return 0

    lax.fori_loop(0, exps * parts, start_wq, 0)
    for e in range(exps):
        arrived(dn1_in.at[e], dn1_sem.at[RECV, e])
    n1_grad = dn1_in[0].astype(full)
    for e in range(1, exps):
        n1_grad = n1_grad + dn1_in[e].astype(full)
    x = tokens[...].astype(full)
    r1 = lax.rsqrt(jnp.mean(x * x, axis=1, keepdims=True) + eps_norm)
    scaled = n1_grad * gains[0:1, :]
    token_grad[...] = (
        dh1[...] + r1 * scaled - x * (r1 * r1 * r1) * jnp.mean(scaled * x, axis=1, keepdims=True)
    )
    small_send[exps : exps + 1, :] = jnp.sum(n1_grad * x * r1, axis=0, keepdims=True)

    line_lane = lane_of((8, 128))
    line_row = row_of((8, 128))
    bias_line = jnp.zeros((8, 128), full)
    flip = jnp.where(row_of((rows, rows)) + lane_of((rows, rows)) == rows - 1, 1.0, 0.0).astype(low)
    turned_bucket = bucket_of(rows - 1 - lane_of((8, span)))
    for h in range(heads):
        high = bias_sum[h].astype(low)
        rest = (bias_sum[h] - high.astype(full)).astype(low)
        flipped = dot(high, flip) + dot(rest, flip)
        square = jnp.concatenate([flipped, jnp.zeros((rows, rows), full)], axis=1)
        turned = pltpu.roll(square, 0, 1, stride=1, stride_axis=0)
        sums = jnp.broadcast_to(jnp.sum(turned, axis=0, keepdims=True), (8, span))
        for b in range(BUCKETS):
            value = jnp.sum(jnp.where(turned_bucket == b, sums, 0.0), axis=1, keepdims=True)
            bias_line = jnp.where(jnp.logical_and(line_row == h, line_lane == b), value, bias_line)
    for h in range(heads):
        small_send[exps + 2 : exps + 3, h * 128 : (h + 1) * 128] = bias_line[h : h + 1, :]

    def small_copies():
        return [
            send(
                small_send,
                small_exp.at[at.exp],
                small_sem.at[SEND, exp_peer(k)],
                small_sem.at[RECV, at.exp],
                at.device(at.rep, exp_peer(k)),
            )
            for k in range(1, exps)
        ]

    for copy in small_copies():
        copy.start()
    small_exp[at.exp] = small_send[...]
    for k in range(1, exps):
        arrived(small_exp.at[exp_peer(k)], small_sem.at[RECV, exp_peer(k)])
    total = small_exp[0]
    for e in range(1, exps):
        total = total + small_exp[e]
    small_sum[0] = total
    for e in range(exps):
        small_sum[0, exps + 3 + e : exps + 4 + e, :] = small_exp[e, exps + 2 : exps + 3, :]

    def small2_copies():
        return [
            send(
                small_sum.at[0],
                small_rep.at[at.rep],
                small2_sem.at[SEND, (at.rep + k) % reps],
                small2_sem.at[RECV, at.rep],
                at.device((at.rep + k) % reps, at.exp),
            )
            for k in range(1, reps)
        ]

    for copy in small2_copies():
        copy.start()
    small_rep[at.rep] = small_sum[0]
    for k in range(1, exps):
        arrived(blk_in.at[exp_peer(k)], blk_sem.at[RECV, exp_peer(k)])
    chosen = jnp.zeros((rows, width), full)
    for e in range(exps):
        chosen = jnp.where(deal[at.base + e] == at.me, blk_in[e].astype(full), chosen)
    block_out[...] = chosen.astype(low)
    for k in range(1, reps):
        arrived(small_rep.at[(at.rep + k) % reps], small2_sem.at[RECV, (at.rep + k) % reps])
    total = small_rep[0]
    for r in range(1, reps):
        total = total + small_rep[r]
    rates = [rate / math.sqrt(width) for rate in (1.5, 6.0, 1.0)]

    def update(i, grad, rate, decay):
        weight, first, second = [state[...] for state in states[3 * i : 3 * i + 3]]
        for new, value in zip(
            news[3 * i : 3 * i + 3], adamw_update(weight, first, second, grad, rate, decay), strict=True
        ):
            new[...] = value

    update(3, total[0:exps], rates[2], 0.1)
    update(4, total[exps : exps + 2], 0.5, 0.0)
    for e in range(exps):
        for h in range(heads):
            bias_grad[e * heads + h : e * heads + h + 1, :] = total[
                exps + 3 + e : exps + 4 + e, h * 128 : h * 128 + BUCKETS
            ]
    update(2, bias_grad[...], 0.3, 0.0)

    for r in range(reps):
        arrived(out_parts.at[r], og_sem.at[RECV, r])
    grad = out_parts[0].astype(full)
    for r in range(1, reps):
        grad = grad + out_parts[r].astype(full)
    update(1, grad, rates[1], 0.1)

    def wq_in(i, _):
        arrived(qkv_parts.at[i // segs, i % segs], wq_sem.at[RECV, i])
        return 0

    lax.fori_loop(0, reps * segs, wq_in, 0)
    grads = []
    for k in range(segs):
        grad = qkv_parts[0, k].astype(full)
        for r in range(1, reps):
            grad = grad + qkv_parts[r, k].astype(full)
        grads.append(grad.T)
    update(0, jnp.concatenate(grads, axis=1), rates[0], 0.1)
    for home in homes:
        home.arrive()

    def sent_c(k, _):
        c_copy(k)[1].wait_send()
        return 0

    lax.fori_loop(1, members, sent_c, 0)
    dn.finish()
    ys.finish()

    for home in homes:
        home.sent()

    def sent_wq(i, _):
        stays, away, _ = wq_copy(i)

        @pl.when(jnp.logical_not(stays))
        def _():
            away().wait_send()

        return 0

    lax.fori_loop(0, exps * parts, sent_wq, 0)
    for copies in (
        do_copies(),
        dz_copies(),
        og_copies(),
        small_copies(),
        blk_copies(),
        small2_copies(),
    ):
        for copy in copies:
            copy.wait_send()
    for k in range(1, exps):
        arrived(dn1_send.at[exp_peer(k)], dn1_sem.at[SEND, exp_peer(k)])


def routed(routes_t, seq, rows):
    pair = routes_t[:, pl.ds(pl.multiple_of(seq * rows, rows), rows)].astype(full)
    cols = jnp.concatenate([pair, jnp.zeros((126, rows), full)], axis=0).T
    lane = lane_of((rows, 128)).astype(full)
    return jnp.logical_or(lane == cols[:, 0:1], lane == cols[:, 1:2])


def backward_call(
    grps, exps, lengths, deal, bias_table, n_parts, y_parts, c_parts, both_g, down_g, in_before, down_before, n1,
    cot_all, routes_t, tokens, h1, n2, probs, qkv, lse, mine, wqkv, wout, states
):
    reps = grps * QUAD
    rows, width = tokens.shape
    heads = HEADS // exps
    head_cols = width // exps
    row_block = wqkv.shape[2]
    out_cols = wout.shape[3]
    shard_cols = 3 * width // reps
    seg = math.gcd(shard_cols, head_cols)
    segs = shard_cols // seg
    parts = 3 * head_cols // seg
    members = QUAD * exps
    chip_bits = bits_of(members) - 1
    small_rows = -(-(2 * exps + 3) // 8) * 8
    shape = jax.ShapeDtypeStruct
    vmem = pl.BlockSpec(memory_space=pltpu.VMEM)
    smem = pl.BlockSpec(memory_space=pltpu.SMEM)
    hbm = pl.BlockSpec(memory_space=pl.ANY)
    results = [
        (shape((rows, width), full), vmem),
        (shape((rows, width), low), vmem),
        (shape(in_before.shape, low), hbm),
        (shape(down_before.shape, low), hbm),
    ] + [(shape(state.shape, full), vmem) for state in states]
    dma = pltpu.SemaphoreType.DMA
    bufs = [pltpu.VMEM((1 << (chip_bits - s), rows, width), low) for s in range(chip_bits + 1)]
    return pl.pallas_call(
        functools.partial(backward_kernel, grps, exps),
        out_shape=[r[0] for r in results],
        in_specs=[smem] * 3 + [hbm] * 9 + [vmem] * 25,
        out_specs=[r[1] for r in results],
        scratch_shapes=[
            pltpu.VMEM((members // 2, rows, width), low),
            list(bufs),
            list(bufs),
            pltpu.VMEM((members, 8, rows), full),
            pltpu.VMEM((rows, width), full),
            pltpu.VMEM((rows, width), low),
            pltpu.VMEM((exps, rows, width), low),
            pltpu.VMEM((exps, rows, head_cols), low),
            pltpu.VMEM((exps, rows, head_cols), low),
            pltpu.VMEM((heads, rows, rows), full),
            pltpu.VMEM((heads, rows, rows), full),
            pltpu.VMEM((rows, 3 * head_cols), low),
            pltpu.VMEM((3 * head_cols, exps * rows), low),
            pltpu.VMEM((exps, rows, width), low),
            pltpu.VMEM((exps, rows, width), low),
            pltpu.VMEM((exps, parts, seg, row_block), low),
            pltpu.VMEM((reps, row_block, out_cols), low),
            pltpu.VMEM((reps, segs, seg, row_block), low),
            pltpu.VMEM((reps, row_block, out_cols), low),
            pltpu.VMEM((rows, width), low),
            pltpu.VMEM((exps, rows, width), low),
            pltpu.VMEM((small_rows, width), full),
            pltpu.VMEM((exps, small_rows, width), full),
            pltpu.VMEM((1, small_rows, width), full),
            pltpu.VMEM((reps, small_rows, width), full),
            pltpu.VMEM((HEADS, BUCKETS), full),
            dma((2, 2, 3 << chip_bits)),
            dma((2, 2, 3 << chip_bits)),
            dma((2, members // 2)),
            dma((2, members)),
            dma((2, 2, 2 * reps)),
            dma((2, 2, max(QUAD, grps))),
            dma((2, exps)),
            dma((2, exps)),
            dma((2, exps)),
            dma((2, max(exps * parts, reps * segs))),
            dma((2, reps)),
            dma((2, exps)),
            dma((2, exps)),
            dma((2, reps)),
            dma((2,)),
        ],
        compiler_params=pltpu.CompilerParams(
            collective_id=1, has_side_effects=True, vmem_limit_bytes=60 * 1024 * 1024
        ),
        input_output_aliases={8: 2, 9: 3},
        name="backward",
    )(
        lengths, deal, bias_table, n_parts, y_parts, c_parts, both_g, down_g, in_before, down_before, n1, cot_all,
        routes_t, tokens, h1, n2, probs, qkv, lse, mine, wqkv, wout, *states
    )


def per_device(
    tokens,
    cotangent,
    seq_lengths,
    deal,
    routes,
    attn_qkv,
    qkv_first,
    qkv_second,
    attn_out,
    out_first,
    out_second,
    rel_bias,
    bias_first,
    bias_second,
    router,
    router_first,
    router_second,
    norm_gains,
    gains_first,
    gains_second,
    expert_in,
    in_first,
    in_second,
    expert_out,
    down_first,
    down_second,
):
    rows, width = tokens.shape
    experts = router.shape[1]
    capacity = (10 * rows + 4 * experts - 1) // (4 * experts)
    exps = lax.axis_size("exp")
    grps = lax.axis_size("grp")
    in_low = expert_in[0].astype(low)
    down_low = expert_out[0].astype(low)
    routes_t = routes.T
    bias_table = rel_bias.T
    (
        both_w, down_w, cot_all, n_all, comb_all, qkv, lse, context_mine, normed_group, wqkv, wout, hidden_one,
        normed_two, router_probs,
    ) = forward_call(
        grps, exps, seq_lengths, bias_table, routes_t, tokens, cotangent, norm_gains.T, router.T,
        attn_qkv.astype(low).T, attn_out.astype(low), in_low, down_low,
    )
    n_parts, y_parts, c_parts, both_g, down_g, in_before, down_before = expert_call(
        grps, exps, capacity, deal, routes_t, comb_all, n_all, cot_all, both_w, down_w, in_low, down_low
    )
    small_states = [
        attn_qkv, qkv_first, qkv_second, attn_out, out_first, out_second, bias_table, bias_first.T, bias_second.T,
        router.T, router_first.T, router_second.T, norm_gains.T, gains_first.T, gains_second.T,
    ]
    token_grad, block_out, in_parts, down_parts, *new = backward_call(
        grps, exps, seq_lengths, deal, bias_table, n_parts, y_parts, c_parts, both_g, down_g, in_before, down_before,
        normed_group, cot_all, routes_t, tokens, hidden_one, normed_two, router_probs, qkv, lse, context_mine, wqkv,
        wout, small_states,
    )
    new = new[:6] + [array.T for array in new[6:]]
    down_share = jnp.sum(down_parts.astype(full), axis=0)[None]
    in_share = jnp.sum(in_parts.astype(full), axis=0)[None]
    in_new = adamw_update(expert_in, in_first, in_second, in_share, 1.5 / math.sqrt(D), 0.1)
    down_new = adamw_update(
        expert_out, down_first, down_second, down_share, 1.5 / math.sqrt(FF), 0.1
    )
    return (block_out, token_grad, *new, *in_new, *down_new)


def bucket_onehot(length):
    places = jnp.arange(length, dtype=jnp.int32)
    offset = places[None, :] - places[:, None]
    distance = jnp.abs(offset)
    bucket = 16 * (offset > 0).astype(jnp.int32)
    for threshold in thresholds:
        bucket = bucket + (distance >= threshold).astype(jnp.int32)
    return (bucket[:, :, None] == jnp.arange(BUCKETS, dtype=jnp.int32)[None, None, :]).astype(full)


def swap(pieces, axes):
    return lax.all_to_all(pieces, axes, split_axis=0, concat_axis=0, tiled=True)


def spread(block, axes):
    members = lax.axis_size(axes)
    return swap(jnp.broadcast_to(block[None], (members,) + block.shape), axes)


def plain_device(
    tokens,
    cotangent,
    seq_lengths,
    deal,
    routes,
    attn_qkv,
    qkv_first,
    qkv_second,
    attn_out,
    out_first,
    out_second,
    rel_bias,
    bias_first,
    bias_second,
    router,
    router_first,
    router_second,
    norm_gains,
    gains_first,
    gains_second,
    expert_in,
    in_first,
    in_second,
    expert_out,
    down_first,
    down_second,
):
    rows, width = tokens.shape
    head_dim = width // HEADS
    score_scale = 1.0 / math.sqrt(head_dim)
    experts = router.shape[1]
    capacity = (10 * rows + 4 * experts - 1) // (4 * experts)
    exps = lax.axis_size("exp")
    grps = lax.axis_size("grp")
    reps = grps * QUAD
    heads = HEADS // exps
    head_cols = heads * head_dim
    place = lax.axis_index("exp")
    base = lax.axis_index(REP) * exps
    me = base + place
    slab = expert_in.shape[1]
    units = expert_out.shape[1]
    quarter = grps * units

    row_block = attn_qkv.shape[0]
    qkv_rows = lax.all_gather(attn_qkv.astype(low), REP, axis=1, tiled=True)
    out_rows = lax.all_gather(attn_out.astype(low), REP, axis=1, tiled=True)
    qkv_pieces = jnp.transpose(
        qkv_rows.reshape(row_block, 3, exps, head_cols), (2, 0, 1, 3)
    ).reshape(exps, row_block, 3 * head_cols)
    qkv_mine = swap(qkv_pieces, "exp").reshape(width, 3 * head_cols)
    full_out = spread(out_rows, "exp").reshape(width, width)

    group_tokens = spread(tokens, "exp")
    group_cotangent = spread(cotangent, "exp")
    my_cotangent = lax.dynamic_index_in_dim(group_cotangent, deal[me] - base, 0, keepdims=False)

    my_routes = lax.dynamic_slice_in_dim(routes, me * rows, rows, 0)
    places = jnp.arange(rows, dtype=jnp.int32)
    valid_rows = (places < seq_lengths[me]).astype(full)
    group_lengths = lax.dynamic_slice_in_dim(seq_lengths, base, exps, 0)
    key_ok = places[None, :] < group_lengths[:, None]
    gain_one = norm_gains[:, 0]
    gain_two = norm_gains[:, 1]

    chosen = (my_routes[:, :, None] == jnp.arange(experts, dtype=jnp.int32)[None, None, :]).astype(full)
    flat_routes = my_routes.reshape(-1)
    route_hot = (flat_routes[:, None] == jnp.arange(experts, dtype=jnp.int32)[None, :]).astype(jnp.int32)
    before = jnp.cumsum(route_hot, axis=0) - route_hot
    slot_index = jnp.sum(before * route_hot, axis=-1)
    target = (flat_routes * capacity + slot_index).reshape(rows, 2)
    slots = experts * capacity
    slot_ids = jnp.arange(slots, dtype=jnp.int32)
    place_first = slot_ids[:, None] == target[None, :, 0]
    place_second = slot_ids[:, None] == target[None, :, 1]
    place_any = jnp.logical_or(place_first, place_second).astype(low)

    shard_in = expert_in[0].astype(low).reshape(slab, 2, grps, QUAD, units)
    in_pieces = jnp.transpose(shard_in, (1, 3, 0, 2, 4)).reshape(2, 1, QUAD, slab, quarter)
    in_pieces = jnp.broadcast_to(in_pieces, (2, grps, QUAD, slab, quarter)).reshape(
        2, reps, slab, quarter
    )
    down_mine = spread(expert_out[0].astype(low), "grp").reshape(quarter, width)
    gate_mine = swap(in_pieces[0], REP).reshape(width, quarter)
    up_mine = swap(in_pieces[1], REP).reshape(width, quarter)

    upstream = my_cotangent.astype(full) * valid_rows[:, None]

    def to_experts(block):
        sent = block.reshape((1, experts) + block.shape[1:])
        sent = jnp.broadcast_to(sent, (QUAD,) + sent.shape[1:])
        return swap(sent.reshape((QUAD * experts,) + block.shape[1:]), PLANE)

    def dispatch(values):
        return dot(place_any, values).astype(low).reshape(experts, capacity, width)

    expert_upstream = to_experts(dispatch(upstream.astype(low))).reshape(-1, width)
    active_grad_bare = lax.dot_general(
        expert_upstream, down_mine, (((1,), (1,)), ((), ())), preferred_element_type=full
    )

    x_group = group_tokens.astype(full)
    scale_group = lax.rsqrt(jnp.mean(x_group * x_group, axis=-1, keepdims=True) + eps_norm)
    normed_group = (x_group * scale_group * gain_one).astype(low).reshape(exps * rows, width)
    qkv = dot(normed_group, qkv_mine).astype(low).reshape(exps, rows, 3, heads, head_dim)
    queries = qkv[:, :, 0]
    key_rows = qkv[:, :, 1]
    values = qkv[:, :, 2]
    onehot = bucket_onehot(rows)
    bias_mine = lax.dynamic_slice_in_dim(rel_bias, place * heads, heads, 1)
    bias_table = jnp.einsum("ijb,bh->hij", onehot, bias_mine, precision=highest)

    def scores_of():
        raw = (
            jnp.einsum("sihd,sjhd->shij", queries, key_rows, preferred_element_type=full)
            * score_scale
            + bias_table[None]
        )
        return jnp.where(key_ok[:, None, None, :], raw, -1e30)

    scores = scores_of()
    row_max = jnp.max(scores, axis=-1, keepdims=True)
    log_total = row_max + jnp.log(jnp.sum(jnp.exp(scores - row_max), axis=-1, keepdims=True))
    weights_low = jnp.exp(scores - log_total).astype(low)
    context_mine = (
        jnp.einsum("shij,sjhd->sihd", weights_low, values, preferred_element_type=full)
        .astype(low)
        .reshape(exps, rows, head_cols)
    )
    context = jnp.transpose(swap(context_mine, "exp"), (1, 0, 2)).reshape(rows, width)

    x_float = tokens.astype(full)
    scale_one = lax.rsqrt(jnp.mean(x_float * x_float, axis=-1, keepdims=True) + eps_norm)
    hidden_one = x_float + dot(context, full_out)
    scale_two = lax.rsqrt(jnp.mean(hidden_one * hidden_one, axis=-1, keepdims=True) + eps_norm)
    normed_two = (hidden_one * scale_two * gain_two).astype(low)
    normed_float = normed_two.astype(full)
    router_probs = jax.nn.softmax(jnp.dot(normed_float, router, precision=highest), axis=-1)
    picked = jnp.sum(router_probs[:, None, :] * chosen, axis=-1)
    gate_total = jnp.sum(picked, axis=-1, keepdims=True)
    gate_value = picked / gate_total
    combine = gate_value * valid_rows[:, None]
    combine_slots = jnp.sum(
        jnp.where(place_first, combine[None, :, 0], 0.0)
        + jnp.where(place_second, combine[None, :, 1], 0.0),
        axis=1,
    ).reshape(experts, 1, capacity)

    expert_rows = to_experts(dispatch(normed_two)).reshape(-1, width)
    expert_combine = to_experts(combine_slots).reshape(-1, 1)

    gate_part = dot(expert_rows, gate_mine)
    up_part = dot(expert_rows, up_mine)
    active_float, active_pull = jax.vjp(gated_unit, gate_part, up_part)
    active = active_float.astype(low)
    active_scaled = (active_float * expert_combine).astype(low)
    combine_grad_part = jnp.sum(active_float * active_grad_bare, axis=-1).reshape(
        QUAD * experts, 1, capacity
    )
    gate_part_grad, up_part_grad = active_pull(active_grad_bare * expert_combine)
    gate_part_grad = gate_part_grad.astype(low)
    up_part_grad = up_part_grad.astype(low)
    rows_grad_part = (
        lax.dot_general(gate_part_grad, gate_mine, (((1,), (1,)), ((), ())), preferred_element_type=full)
        + lax.dot_general(up_part_grad, up_mine, (((1,), (1,)), ((), ())), preferred_element_type=full)
    ).astype(low)
    output_part = dot(active, down_mine).astype(low)

    combine_grad_back = swap(combine_grad_part, PLANE)
    rows_grad_back = swap(rows_grad_part.reshape(QUAD * experts, capacity, width), PLANE)
    output_back = swap(output_part.reshape(QUAD * experts, capacity, width), PLANE)

    def transposed_dot(a, b):
        return lax.dot_general(a, b, (((0,), (0,)), ((), ())), preferred_element_type=full)

    down_grad = transposed_dot(active_scaled, expert_upstream).astype(low)
    gate_grad = transposed_dot(expert_rows, gate_part_grad).astype(low)
    up_grad = transposed_dot(expert_rows, up_part_grad).astype(low)
    down_share = jnp.sum(
        swap(down_grad.reshape(grps, units, width), "grp").astype(full), axis=0
    )[None]

    def in_columns(grad):
        back = swap(grad.reshape(reps, slab, quarter), REP).astype(full)
        back = jnp.sum(back.reshape(grps, QUAD, slab, grps, units), axis=0)
        return jnp.transpose(back, (1, 2, 0, 3)).reshape(slab, grps * QUAD * units)

    in_share = jnp.concatenate([in_columns(gate_grad), in_columns(up_grad)], axis=1)[None]

    def from_slots(placed, parts):
        hot = jnp.broadcast_to(placed.astype(low)[None], (QUAD,) + placed.shape).reshape(-1, rows)
        return lax.dot_general(
            hot, parts.reshape(-1, width), (((0,), (0,)), ((), ())), preferred_element_type=full
        )

    mixture = combine[:, :1] * from_slots(place_first, output_back) + combine[:, 1:] * from_slots(
        place_second, output_back
    )
    block_loader = (valid_rows[:, None] * (hidden_one + mixture)).astype(low)
    seq_ids = jnp.arange(deal.shape[0], dtype=jnp.int32)
    dealt_seq = jnp.sum(jnp.where(deal == me, seq_ids, 0))
    block_out = lax.dynamic_index_in_dim(
        spread(block_loader, "exp"), dealt_seq - base, 0, keepdims=False
    )

    combine_grad_slots = jnp.sum(combine_grad_back.reshape(QUAD, slots), axis=0)
    combine_grad = jnp.stack(
        [
            jnp.sum(jnp.where(place_first, combine_grad_slots[:, None], 0.0), axis=0),
            jnp.sum(jnp.where(place_second, combine_grad_slots[:, None], 0.0), axis=0),
        ],
        axis=1,
    )
    gate_grad_value = combine_grad * valid_rows[:, None]
    picked_grad = (
        gate_grad_value - jnp.sum(gate_grad_value * gate_value, axis=-1, keepdims=True)
    ) / gate_total
    probs_grad = jnp.sum(picked_grad[:, :, None] * chosen, axis=1)
    logit_grad = router_probs * (
        probs_grad - jnp.sum(probs_grad * router_probs, axis=-1, keepdims=True)
    )
    router_grad = jnp.dot(normed_float.T, logit_grad, precision=highest)
    normed_grad = jnp.dot(logit_grad, router.T, precision=highest) + from_slots(
        jnp.logical_or(place_first, place_second), rows_grad_back
    )
    scaled_two = normed_grad * gain_two
    hidden_grad = (
        upstream
        + scale_two * scaled_two
        - hidden_one * scale_two**3 * jnp.mean(scaled_two * hidden_one, axis=-1, keepdims=True)
    )
    gain_two_grad = jnp.sum(normed_grad * hidden_one * scale_two, axis=0)
    branch_grad = hidden_grad.astype(low)
    context_grad = lax.dot_general(
        branch_grad, full_out, (((1,), (1,)), ((), ())), preferred_element_type=full
    ).astype(low)
    context_grad_pieces = jnp.transpose(context_grad.reshape(rows, exps, head_cols), (1, 0, 2))
    context_grad_mine = swap(context_grad_pieces, "exp").reshape(exps, rows, heads, head_dim)
    branch_group = spread(branch_grad, "exp").reshape(exps * rows, width)
    out_grad = transposed_dot(context_mine.reshape(exps * rows, head_cols), branch_group).astype(low)

    scores = scores_of()
    probs_again = jnp.exp(scores - log_total)
    weights_again = probs_again.astype(low)
    values_grad = jnp.einsum(
        "shij,sihd->sjhd", weights_again, context_grad_mine, preferred_element_type=full
    )
    probs_grad_att = jnp.einsum(
        "sihd,sjhd->shij", context_grad_mine, values, preferred_element_type=full
    )
    row_delta = jnp.sum(probs_grad_att * probs_again, axis=-1, keepdims=True)
    scores_grad = (probs_again * (probs_grad_att - row_delta)).astype(low)
    scores_grad_sum = jnp.sum(scores_grad.astype(full), axis=0)
    bias_grad_mine = jnp.einsum("hij,ijb->bh", scores_grad_sum, onehot, precision=highest)
    bias_grad = lax.dynamic_update_slice_in_dim(
        jnp.zeros((BUCKETS, HEADS), full), bias_grad_mine, place * heads, 1
    )
    queries_grad = (
        jnp.einsum("shij,sjhd->sihd", scores_grad, key_rows, preferred_element_type=full)
        * score_scale
    )
    keys_grad = (
        jnp.einsum("shij,sihd->sjhd", scores_grad, queries, preferred_element_type=full)
        * score_scale
    )
    qkv_grad = (
        jnp.stack([queries_grad, keys_grad, values_grad], axis=2)
        .astype(low)
        .reshape(exps * rows, 3 * head_cols)
    )
    normed_one_part = lax.dot_general(
        qkv_grad, qkv_mine, (((1,), (1,)), ((), ())), preferred_element_type=full
    ).astype(low)
    normed_one_grad = jnp.sum(
        swap(normed_one_part.reshape(exps, rows, width), "exp").astype(full), axis=0
    )
    scaled_one = normed_one_grad * gain_one
    token_grad = (
        hidden_grad
        + scale_one * scaled_one
        - x_float * scale_one**3 * jnp.mean(scaled_one * x_float, axis=-1, keepdims=True)
    )
    gain_one_grad = jnp.sum(normed_one_grad * x_float * scale_one, axis=0)

    qkv_weight_grad = transposed_dot(normed_group, qkv_grad).astype(low)
    qkv_grad_rows = swap(qkv_weight_grad.reshape(exps, row_block, 3 * head_cols), "exp")
    qkv_grad_rows = jnp.transpose(
        qkv_grad_rows.reshape(exps, row_block, 3, head_cols), (1, 2, 0, 3)
    ).reshape(row_block, reps, -1)
    qkv_share = jnp.sum(
        swap(jnp.transpose(qkv_grad_rows, (1, 0, 2)), REP).astype(full), axis=0
    )
    out_pieces = jnp.transpose(out_grad.reshape(row_block, reps, -1), (1, 0, 2))
    out_share = jnp.sum(swap(out_pieces, REP).astype(full), axis=0)

    small = jnp.concatenate(
        [
            router_grad.reshape(-1),
            jnp.stack([gain_one_grad, gain_two_grad], axis=1).reshape(-1),
            bias_grad.reshape(-1),
        ]
    ).reshape(-1, 128)
    small_total = jnp.sum(lax.all_gather(small, ALL, axis=0, tiled=False), axis=0).reshape(-1)
    router_total = small_total[: router.size].reshape(router.shape)
    gains_total = small_total[router.size : router.size + norm_gains.size].reshape(norm_gains.shape)
    bias_total = small_total[router.size + norm_gains.size :].reshape(rel_bias.shape)

    qkv_new = adamw_update(attn_qkv, qkv_first, qkv_second, qkv_share, 1.5 / math.sqrt(D), 0.1)
    out_new = adamw_update(attn_out, out_first, out_second, out_share, 6.0 / math.sqrt(D), 0.1)
    bias_new = adamw_update(rel_bias, bias_first, bias_second, bias_total, 0.3, 0.0)
    router_new = adamw_update(
        router, router_first, router_second, router_total, 1.0 / math.sqrt(D), 0.1
    )
    gains_new = adamw_update(norm_gains, gains_first, gains_second, gains_total, 0.5, 0.0)
    in_new = adamw_update(expert_in, in_first, in_second, in_share, 1.5 / math.sqrt(D), 0.1)
    down_new = adamw_update(
        expert_out, down_first, down_second, down_share, 1.5 / math.sqrt(FF), 0.1
    )
    return (
        (block_out, token_grad)
        + qkv_new
        + out_new
        + bias_new
        + router_new
        + gains_new
        + in_new
        + down_new
    )


def solution(mesh):
    reps, exps = mesh.devices.shape
    split = Mesh(mesh.devices.reshape(reps // QUAD, QUAD, exps), ALL)
    by_rows = P(ALL, None)
    attn = P("exp", REP)
    expert = P("exp", REP, None)
    return jax.shard_map(
        per_device if (reps, exps) == (2 * QUAD, 4) else plain_device,
        mesh=split,
        in_specs=(by_rows, by_rows) + (P(),) * 3 + (attn,) * 6 + (P(),) * 9 + (expert,) * 6,
        out_specs=(by_rows, by_rows) + (attn,) * 6 + (P(),) * 9 + (expert,) * 6,
        check_vma=False,
    )
```

```python
import functools
import math

import jax
import jax.numpy as jnp
from jax import lax
from jax.experimental import pallas as pl
from jax.experimental.pallas import tpu as pltpu
from jax.sharding import Mesh
from jax.sharding import PartitionSpec as P

D = 1024
HEADS = 16
FF = 2816
BUCKETS = 32
STEP = 10
QUAD = 4
REP = ("grp", "quad")
PLANE = ("quad", "exp")
ALL = ("grp", "quad", "exp")

highest = lax.Precision.HIGHEST
eps_norm = 1e-06
thresholds = (1, 2, 3, 4, 5, 6, 7, 8, 11, 16, 22, 32, 45, 64, 90)
beta_one = 0.9
beta_two = 0.999
eps_adam = 1e-08
low = jnp.bfloat16
full = jnp.float32
MESH = pl.DeviceIdType.MESH


def adamw_update(weight, moment, second, gradient, step_rate, decay_factor):
    new_moment = beta_one * moment + (1.0 - beta_one) * gradient
    new_second = beta_two * second + (1.0 - beta_two) * gradient * gradient
    corrected = new_moment / (1.0 - beta_one**STEP)
    scaled = new_second / (1.0 - beta_two**STEP)
    new_weight = weight - step_rate * (
        corrected / (jnp.sqrt(scaled) + eps_adam) + decay_factor * weight
    )
    return (new_moment, new_second, new_weight)


def gated_unit(gate_input, up_input):
    return jax.nn.gelu(gate_input, approximate=True) * up_input


def dot(a, b):
    return jnp.dot(a, b, preferred_element_type=full)


def nt(a, b, precision=None):
    return lax.dot_general(a, b, (((1,), (1,)), ((), ())), preferred_element_type=full, precision=precision)


def tn(a, b):
    return lax.dot_general(a, b, (((0,), (0,)), ((), ())), preferred_element_type=full)


class Where:
    def __init__(self, grps, exps):
        self.grps, self.exps = grps, exps
        self.reps = grps * QUAD
        self.grp = lax.axis_index("grp")
        self.quad = lax.axis_index("quad")
        self.exp = lax.axis_index("exp")
        self.rep = self.grp * QUAD + self.quad
        self.base = self.rep * exps
        self.me = self.base + self.exp

    def device(self, rep, exp):
        return (rep // QUAD, rep % QUAD, exp)

    def near(self, flip):
        q = self.quad
        if flip & 1:
            q = q + 1 - 2 * (q % 2)
        if flip & 2:
            q = q + 2 - 4 * (q // 2)
        return q


def send(src, dst, send_sem, recv_sem, device):
    return pltpu.make_async_remote_copy(
        src_ref=src, dst_ref=dst, send_sem=send_sem, recv_sem=recv_sem, device_id=device, device_id_type=MESH
    )


def arrived(ref, sem):
    pltpu.make_async_copy(ref, ref, sem).wait()


def greet_all(at):
    count = at.reps * at.exps
    barrier = pltpu.get_barrier_semaphore()

    def greet(k, _):
        other = (at.me + k) % count
        pl.semaphore_signal(
            barrier, inc=1, device_id=at.device(other // at.exps, other % at.exps), device_id_type=MESH
        )
        return 0

    lax.fori_loop(1, count, greet, 0)
    pl.semaphore_wait(barrier, count - 1)


def turn(exp, i):
    beside = exp + 1 - 2 * (exp % 2)
    return jnp.where(i == 0, (beside + 2) % 4, jnp.where(i == 1, (exp + 2) % 4, jnp.where(i == 2, beside, exp)))


def lane_of(shape):
    return lax.broadcasted_iota(jnp.int32, shape, 1)


def row_of(shape):
    return lax.broadcasted_iota(jnp.int32, shape, 0)


def bucket_of(offset):
    distance = jnp.abs(offset)
    bucket = jnp.where(offset > 0, 16, 0)
    for threshold in thresholds:
        bucket = bucket + jnp.where(distance >= threshold, 1, 0)
    return bucket


def bits_of(count):
    return count.bit_length() - 1


def column_parts(width):
    tiles = width // 128
    cuts = [0, (tiles + 2) // 3, (2 * tiles + 2) // 3, tiles]
    return [(cuts[i] * 128, (cuts[i + 1] - cuts[i]) * 128) for i in range(3)]


def flipped(place, bit):
    return place + (1 - 2 * ((place // (1 << bit)) % 2)) * (1 << bit)


class Doubling:
    def __init__(self, at, own, every, sems, core_sems, orders):
        self.at, self.own, self.every = at, own, every
        self.sems, self.core_sems, self.orders = sems, core_sems, orders
        self.plane = at.quad * at.exps + at.exp
        self.steps = len(orders[0])
        self.parts = column_parts(own.shape[1])

    def device(self, bit):
        other = flipped(self.plane, bit)
        return (self.at.grp, other // self.at.exps, other % self.at.exps)

    def place(self, part, j):
        p = self.plane
        for i, bit in enumerate(self.orders[part]):
            if (j >> i) & 1:
                p = flipped(p, bit + 1)
        return p

    def block(self, part, p):
        begin, size = self.parts[part]
        return self.every.at[p, :, pl.ds(begin, size)]

    def source(self, part, j):
        begin, size = self.parts[part]
        return self.own.at[:, pl.ds(begin, size)] if j == 0 else self.block(part, self.place(part, j))

    def index(self, step, part, j):
        return part * (1 << self.steps) + (1 << step) - 1 + j

    def copy(self, step, part, j):
        i = self.index(step, part, j)
        return send(
            self.source(part, j),
            self.block(part, self.place(part, j)),
            self.sems.at[0, i],
            self.sems.at[1, i],
            self.device(self.orders[part][step] + 1),
        )

    def core_copy(self, part, j):
        i = part * (1 << self.steps) + j
        return send(
            self.source(part, j),
            self.block(part, self.place(part, j)),
            self.core_sems.at[0, i],
            self.core_sems.at[1, i],
            self.device(0),
        )

    def start(self):
        for part in range(3):
            for step in range(self.steps):
                self.copy(step, part, 0).start()
        for part in range(3):
            self.core_copy(part, 0).start()
        self.keep().start()

    def keep(self):
        return pltpu.make_async_copy(self.own, self.every.at[self.plane], self.core_sems.at[1, 3 << self.steps])

    def next(self, step):
        for part in range(3):
            for j in range(1 << step):
                k = (1 << step) + j
                arrived(self.block(part, self.place(part, k)), self.sems.at[1, self.index(step, part, j)])
                for later in range(step + 1, self.steps):
                    self.copy(later, part, k).start()
                self.core_copy(part, k).start()

    def finish_in(self):
        for part in range(3):
            for j in range(1 << self.steps):
                there = self.block(part, flipped(self.place(part, j), 0))
                arrived(there, self.core_sems.at[1, part * (1 << self.steps) + j])
        self.keep().wait()

    def finish_out(self):
        for part in range(3):
            for j in range(1 << self.steps):
                self.core_copy(part, j).wait_send()
            for step in range(self.steps):
                for j in range(1 << step):
                    self.copy(step, part, j).wait_send()


class Group:
    def __init__(self, at, own, every, sems):
        self.at, self.own, self.every, self.sems = at, own, every, sems
        self.beside, self.across = at.exp + 1 - 2 * (at.exp % 2), (at.exp + 2) % 4

    def copy(self, src, index, send_index, device):
        return send(
            src, self.every.at[index], self.sems.at[0, send_index], self.sems.at[1, index], self.at.device(self.at.rep, device)
        )

    def first(self):
        return [
            self.copy(self.own, self.at.exp, 0, self.across),
            self.copy(self.own, self.at.exp, 1, self.beside),
        ]

    def second(self):
        return self.copy(self.every.at[self.across], self.across, 2, self.beside)

    def start(self):
        for copy in self.first():
            copy.start()

    def pass_on(self):
        arrived(self.every.at[self.across], self.sems.at[1, self.across])
        self.second().start()

    def arrive(self):
        for index in (self.beside, (self.beside + 2) % 4):
            arrived(self.every.at[index], self.sems.at[1, index])

    def sent(self):
        for copy in self.first() + [self.second()]:
            copy.wait_send()


class Tiles:
    def __init__(self, units, reps):
        self.units = units
        self.reps = reps
        self.hidden = units * reps
        self.half = self.hidden // 256
        self.wide = (self.half + 1) // 2
        self.count = 3
        self.size = 128 * self.wide // self.count
        self.skip = 128 * (2 * self.wide - self.half)

    def start(self, quad):
        return 128 * (self.half * (quad // 2) + (self.half - self.wide) * (quad % 2))

    def rows(self, tile):
        result = []
        for k in range(QUAD):
            found = None
            for parity in range(2):
                first = self.start(parity) + tile * self.size
                live = first + (self.skip if parity and tile == 0 else 0)
                begin = max(live, k * self.units)
                end = min(first + self.size, (k + 1) * self.units)
                if end > begin:
                    found = (begin - k * self.units, end - begin, parity, begin - first)
            result.append(found)
        return result


class Outward:
    def __init__(self, at, tiles, tile, in_low, down_slab, both_w, down_w, nothing, sems, down_sems):
        self.at, self.tiles, self.tile = at, tiles, tile
        self.in_low, self.down_slab, self.both_w, self.down_w = in_low, down_slab, both_w, down_w
        self.nothing, self.sems, self.down_sems = nothing, sems, down_sems
        self.slab = in_low.shape[0]

    def source(self, quad, section):
        begin = section * self.tiles.hidden + self.tiles.start(quad) + self.tile * self.tiles.size
        return self.in_low.at[:, pl.ds(pl.multiple_of(begin, 128), self.tiles.size)]

    def target(self, rep, section):
        rows = pl.ds(pl.multiple_of(rep * self.slab, self.slab), self.slab)
        return self.both_w.at[rows, pl.ds(section * self.tiles.size, self.tiles.size)]

    def over(self, act):
        at = self.at

        def one(k, _):
            other = (at.rep + k) % at.reps
            for section in range(2):
                act(
                    functools.partial(
                        send,
                        self.source(other % QUAD, section),
                        self.target(at.rep, section),
                        self.sems.at[0, section * at.reps + other],
                        self.sems.at[1, section * at.reps + at.rep],
                        at.device(other, at.exp),
                    )
                )
            return 0

        lax.fori_loop(1, at.reps, one, 0)

    def over_down(self, act, act_local):
        at = self.at
        for k, piece in enumerate(self.tiles.rows(self.tile)):
            if piece is None:
                continue
            begin, count, parity, to = piece
            quad = 2 * (at.rep // QUAD) + parity
            src, dst = self.down_slab.at[pl.ds(begin, count)], self.down_w.at[pl.ds(to, count)]
            recv = self.down_sems.at[1, at.rep]
            for g in range(at.grps):
                stays = jnp.logical_and(at.grp == g, at.quad == quad)
                ours = at.rep % QUAD == k

                @pl.when(jnp.logical_and(ours, jnp.logical_not(stays)))
                def _():
                    act(functools.partial(send, src, dst, self.down_sems.at[0, g], recv, (g, quad, at.exp)))

                @pl.when(jnp.logical_and(ours, stays))
                def _():
                    act_local(functools.partial(pltpu.make_async_copy, src, dst, recv))

    def blank(self):
        return pltpu.make_async_copy(
            self.nothing, self.down_w.at[pl.ds(0, self.tiles.skip)], self.down_sems.at[1, self.at.reps]
        )

    def start(self):
        at = self.at
        self.over_down(lambda copy: copy().start(), lambda copy: copy().start())
        self.over(lambda copy: copy().start())
        for section in range(2):
            pltpu.make_async_copy(
                self.source(at.quad, section), self.target(at.rep, section), self.sems.at[1, section * at.reps + at.rep]
            ).start()
        if self.tile == 0:

            @pl.when(at.quad % 2 == 1)
            def _():
                self.blank().start()

    def arrive(self):
        at = self.at

        def one(rep, _):
            for section in range(2):
                arrived(self.target(rep, section), self.sems.at[1, section * at.reps + rep])
            return 0

        lax.fori_loop(0, at.reps, one, 0)
        for parity in range(2):

            @pl.when(at.quad % 2 == parity)
            def _():
                for k, piece in enumerate(self.tiles.rows(self.tile)):
                    if piece is not None and piece[2] == parity:
                        source = QUAD * (at.quad // 2) + k
                        arrived(self.down_w.at[pl.ds(piece[3], piece[1])], self.down_sems.at[1, source])
                if parity and self.tile == 0:
                    self.blank().wait()

    def sent(self):
        self.over(lambda copy: copy().wait_send())
        self.over_down(lambda copy: copy().wait_send(), lambda copy: None)


class Homeward:
    def __init__(self, at, tiles, tile, both, down, in_parts, down_parts, sems, down_sems):
        self.at, self.tiles, self.tile = at, tiles, tile
        self.both, self.down, self.in_parts, self.down_parts = both, down, in_parts, down_parts
        self.sems, self.down_sems = sems, down_sems
        self.slab = in_parts.shape[1]

    def target(self, grp, quad, parity, section):
        skip = self.tiles.skip if parity and self.tile == 0 else 0
        to = section * self.tiles.hidden + self.tiles.start(quad) + self.tile * self.tiles.size + skip
        to = to if isinstance(to, int) else pl.multiple_of(to, 128)
        return skip, self.in_parts.at[grp, :, pl.ds(to, self.tiles.size - skip)]

    def copy(self, rep, parity, section, local=False):
        at = self.at
        skip, dst = self.target(at.grp, at.quad, parity, section)
        rows = pl.ds(pl.multiple_of(rep * self.slab, self.slab), self.slab)
        src = self.both.at[rows, pl.ds(section * self.tiles.size + skip, self.tiles.size - skip)]
        recv = self.sems.at[1, section * at.reps + at.rep]
        if local:
            return pltpu.make_async_copy(src, dst, recv)
        return send(src, dst, self.sems.at[0, section * at.reps + rep], recv, at.device(rep, at.exp))

    def over(self, act, act_local):
        at = self.at
        for parity in range(2):

            @pl.when(at.quad % 2 == parity)
            def _():
                def one(k, _):
                    for section in range(2):
                        act(self.copy((at.rep + k) % at.reps, parity, section))
                    return 0

                lax.fori_loop(1, at.reps, one, 0)
                if act_local:
                    for section in range(2):
                        act_local(self.copy(at.rep, parity, section, local=True))

    def over_down(self, act, act_local):
        at = self.at
        for k, piece in enumerate(self.tiles.rows(self.tile)):
            if piece is None:
                continue
            begin, count, parity, to = piece
            src, dst = self.down.at[pl.ds(to, count)], self.down_parts.at[at.grp, pl.ds(begin, count)]
            recv = self.down_sems.at[1, at.grp]
            stays = jnp.logical_and(at.grp == at.quad // 2, at.quad == k)
            ours = at.quad % 2 == parity

            @pl.when(jnp.logical_and(ours, jnp.logical_not(stays)))
            def _():
                act(functools.partial(send, src, dst, self.down_sems.at[0, k], recv, (at.quad // 2, k, at.exp)))

            @pl.when(jnp.logical_and(ours, stays))
            def _():
                act_local(functools.partial(pltpu.make_async_copy, src, dst, recv))

    def start(self):
        self.over_down(lambda copy: copy().start(), lambda copy: copy().start())
        self.over(lambda copy: copy.start(), lambda copy: copy.start())

    def arrive(self):
        at = self.at
        for rep in range(at.reps):
            for section in range(2):
                _, dst = self.target(rep // QUAD, rep % QUAD, rep % 2, section)
                arrived(dst, self.sems.at[1, section * at.reps + rep])
        for k, piece in enumerate(self.tiles.rows(self.tile)):
            if piece is None:
                continue

            @pl.when(at.quad == k)
            def _():
                for g in range(at.grps):
                    arrived(self.down_parts.at[g, pl.ds(piece[0], piece[1])], self.down_sems.at[1, g])

    def sent(self):
        self.over(lambda copy: copy.wait_send(), None)
        self.over_down(lambda copy: copy().wait_send(), lambda copy: None)


def forward_kernel(
    grps,
    exps,
    lengths,
    bias_table,
    routes_t,
    tokens,
    cotangent,
    gains,
    router,
    qkv_t,
    out_w,
    in_low,
    down_slab,
    both_w,
    down_w,
    cot_all,
    n_all,
    comb_all,
    qkv_out,
    lse_out,
    mine_out,
    n1_out,
    wqkv_out,
    wout_out,
    h1_out,
    n2_out,
    probs_out,
    tok_all,
    wqkv,
    wout,
    n1,
    qkv,
    lse,
    mine,
    ctx,
    bias,
    comb_send,
    nothing,
    tok_sem,
    wq_sem,
    wo_sem,
    wo2_sem,
    weight_sem,
    down_sem,
    ctx_sem,
    cot_sem,
    cot_core_sem,
    n_sem,
    n_core_sem,
    comb_sem,
    store_sem,
):
    at = Where(grps, exps)
    reps = at.reps
    rows, width = tokens.shape
    heads = HEADS // exps
    head_dim = width // HEADS
    head_cols = heads * head_dim
    block_cols = min(128, head_cols)
    shard_cols, row_block = qkv_t.shape
    seg = math.gcd(shard_cols, head_cols)
    segs = shard_cols // seg
    tiles = Tiles(down_slab.shape[0], reps)
    plane = at.quad * exps + at.exp
    members = QUAD * exps
    scale = 1.0 / math.sqrt(head_dim)
    SEND, RECV = 0, 1

    greet_all(at)

    def exp_peer(k):
        return (at.exp + k) % exps

    group_tokens = Group(at, tokens, tok_all, tok_sem)
    group_tokens.start()
    tok_all[at.exp] = tokens[...]

    def segment(k):
        col = (at.rep * segs + k) * seg
        section = col // width
        within = col - section * width
        owner = within // head_cols
        return owner, section * head_cols + within - owner * head_cols

    def segment_copy(k, shift):
        owner, offset = segment(k)
        src = qkv_t.at[pl.ds(k * seg, seg)]
        dst = wqkv.at[at.exp, pl.ds(pl.multiple_of(offset, seg), seg)]
        target = at.device((at.rep + shift) % reps, owner)
        return owner, src, dst, functools.partial(
            send, src, dst, wq_sem.at[SEND, k * reps + shift], wq_sem.at[RECV, at.exp * 3 * (head_cols // seg) + offset // seg], target
        )

    def over_segments(act, act_local):
        def one(i, _):
            k, shift = i // reps, i % reps
            owner, src, dst, copy = segment_copy(k, shift)
            stays = jnp.logical_and(shift == 0, owner == at.exp)

            @pl.when(jnp.logical_not(stays))
            def _():
                act(copy())

            @pl.when(stays)
            def _():
                act_local(k, src, dst)

            return 0

        lax.fori_loop(0, segs * reps, one, 0)

    def local_segment(k, src, dst):
        _, offset = segment(k)
        pltpu.make_async_copy(src, dst, wq_sem.at[RECV, at.exp * 3 * (head_cols // seg) + offset // seg]).start()

    over_segments(lambda copy: copy.start(), local_segment)

    for k in range(1, reps):
        other = (at.rep + k) % reps
        send(
            out_w, wout.at[at.exp, at.rep], wo_sem.at[SEND, other], wo_sem.at[RECV, at.rep], at.device(other, at.exp)
        ).start()
    wout[at.exp, at.rep] = out_w[...]
    chip_bits = list(range(bits_of(members) - 1))
    cots = Doubling(at, cotangent, cot_all, cot_sem, cot_core_sem, [chip_bits[::-1]] * 3)
    cots.start()

    span = 2 * rows
    bucket = bucket_of(lane_of((8, span)) - rows)
    for h in range(heads):
        line = jnp.zeros((8, span), full)
        for b in range(BUCKETS):
            line = jnp.where(bucket == b, bias_table[at.exp * heads + h, b], line)
        whole = jnp.broadcast_to(line[0:1], (rows, span))
        bias[h] = pltpu.roll(whole, 0, 1, stride=1, stride_axis=0)[:, rows:]

    group_tokens.pass_on()
    group_tokens.arrive()

    def norm_group(s, _):
        x = tok_all[s].astype(full)
        r = lax.rsqrt(jnp.mean(x * x, axis=1, keepdims=True) + eps_norm)
        n1[s] = (x * r * gains[0:1, :]).astype(low)
        return 0

    lax.fori_loop(0, exps, norm_group, 0)

    nothing[...] = jnp.zeros_like(nothing)
    weights = [
        Outward(
            at, tiles, t, in_low, down_slab, both_w.at[t], down_w.at[t], nothing, weight_sem.at[t], down_sem.at[t]
        )
        for t in range(2)
    ]
    weights[0].start()

    def wait_segment(i, _):
        e, j = i // (3 * head_cols // seg), i % (3 * head_cols // seg)
        arrived(wqkv.at[e, pl.ds(pl.multiple_of(j * seg, seg), seg)], wq_sem.at[RECV, i])
        return 0

    lax.fori_loop(0, exps * 3 * head_cols // seg, wait_segment, 0)

    def project(s, _):
        total = jnp.zeros((rows, 3 * head_cols), full)
        for e in range(exps):
            total = total + nt(n1[s, :, e * row_block : (e + 1) * row_block], wqkv[e])
        qkv[s] = total.astype(low)
        return 0

    lax.fori_loop(0, exps, project, 0)

    for k in range(1, reps):
        other = (at.rep + k) % reps
        arrived(wout.at[at.exp, other], wo_sem.at[RECV, other])

    group_wout = Group(at, wout.at[at.exp], wout, wo2_sem)
    group_wout.start()
    cots.next(0)

    def attend(i, _):
        s = turn(at.exp, i)
        ok = lane_of((rows, rows)) < lengths[at.base + s]
        lane = lane_of((rows, block_cols))
        sums = jnp.zeros((rows, 128), full)
        for c in range(head_cols // block_cols):
            cols = slice(c * block_cols, (c + 1) * block_cols)
            q = qkv[s, :, cols]
            k = qkv[s, :, head_cols + c * block_cols : head_cols + (c + 1) * block_cols]
            v = qkv[s, :, 2 * head_cols + c * block_cols : 2 * head_cols + (c + 1) * block_cols]
            result = jnp.zeros((rows, block_cols), full)
            for t in range(block_cols // head_dim):
                h = c * (block_cols // head_dim) + t
                here = jnp.logical_and(lane >= t * head_dim, lane < (t + 1) * head_dim)
                scores = nt(jnp.where(here, q, jnp.zeros_like(q)), k) * scale + bias[h]
                scores = jnp.where(ok, scores, -1e30)
                top = jnp.max(scores, axis=1, keepdims=True)
                weights = jnp.exp(scores - top)
                total = jnp.sum(weights, axis=1, keepdims=True)
                weights = (weights * (1.0 / total)).astype(low)
                result = jnp.where(here, jnp.dot(weights, v, preferred_element_type=full), result)
                sums = jnp.where(lane_of((rows, 128)) == h, top + jnp.log(total), sums)
            mine[s, :, cols] = result.astype(low)
        lse[s] = sums

        @pl.when(i < exps - 1)
        def _():
            send(
                mine.at[s], ctx.at[at.exp], ctx_sem.at[SEND, s], ctx_sem.at[RECV, at.exp], at.device(at.rep, s)
            ).start()

        @pl.when(i == exps - 1)
        def _():
            pltpu.make_async_copy(mine.at[s], ctx.at[at.exp], ctx_sem.at[RECV, at.exp]).start()

        return 0

    lax.fori_loop(0, exps, attend, 0)

    group_wout.pass_on()
    cots.next(1)
    group_wout.arrive()
    for e in range(exps):
        arrived(ctx.at[e], ctx_sem.at[RECV, e])

    out_cols = wout.shape[3]
    for r in range(reps):
        cols = slice(r * out_cols, (r + 1) * out_cols)
        total = tokens[:, cols].astype(full)
        for e in range(exps):
            total = total + jnp.dot(ctx[e], wout[e, r], preferred_element_type=full)
        h1_out[:, cols] = total
    h1 = h1_out[...]
    r2 = lax.rsqrt(jnp.mean(h1 * h1, axis=1, keepdims=True) + eps_norm)
    n2 = (h1 * r2 * gains[1:2, :]).astype(low)
    n2_out[...] = n2
    rotated = [chip_bits[c:] + chip_bits[:c] for c in range(3)]
    rows_two = Doubling(at, n2_out, n_all, n_sem, n_core_sem, rotated)
    rows_two.start()
    weights[1].start()

    router_rows = jnp.concatenate([router[...], jnp.zeros((128 - exps, width), full)], axis=0)
    logits = nt(n2.astype(full), router_rows, precision=highest)
    lane = lane_of((rows, 128))
    logits = jnp.where(lane < exps, logits, -1e30)
    probs = jnp.exp(logits - jnp.max(logits, axis=1, keepdims=True))
    probs = probs / jnp.sum(probs, axis=1, keepdims=True)
    probs_out[...] = probs
    picked = jnp.where(routed(routes_t, at.me, rows), probs, 0.0)
    comb = picked / jnp.sum(picked, axis=1, keepdims=True)
    comb = jnp.where(row_of((rows, 1)) < lengths[at.me], comb, 0.0)
    comb_send[...] = comb.T[0 : comb_send.shape[0]]

    def comb_copy(k):
        other = (plane + k) % members
        return send(
            comb_send,
            comb_all.at[plane],
            comb_sem.at[SEND, other],
            comb_sem.at[RECV, plane],
            (at.grp, other // exps, other % exps),
        )

    def start_comb(k, _):
        comb_copy(k).start()
        return 0

    lax.fori_loop(1, members, start_comb, 0)
    pltpu.make_async_copy(comb_send, comb_all.at[plane], comb_sem.at[RECV, plane]).start()
    rows_two.next(0)

    stores = [
        (qkv, qkv_out),
        (lse, lse_out),
        (mine, mine_out),
        (n1, n1_out),
        (wqkv, wqkv_out),
        (wout, wout_out),
    ]
    for i, (src, dst) in enumerate(stores):
        pltpu.make_async_copy(src, dst, store_sem.at[i]).start()

    for step in range(1, rows_two.steps):
        rows_two.next(step)
    for step in range(2, cots.steps):
        cots.next(step)

    cots.finish_in()
    rows_two.finish_in()

    def comb_in(k, _):
        arrived(comb_all.at[k], comb_sem.at[RECV, k])
        return 0

    lax.fori_loop(0, members, comb_in, 0)
    for tile in weights:
        tile.arrive()

    for k in range(1, exps):
        peer = exp_peer(k)
        arrived(mine.at[peer], ctx_sem.at[SEND, peer])
    over_segments(lambda copy: copy.wait_send(), lambda k, src, dst: None)
    for k in range(1, reps):
        arrived(out_w, wo_sem.at[SEND, (at.rep + k) % reps])
    group_tokens.sent()
    group_wout.sent()
    cots.finish_out()
    rows_two.finish_out()

    def sent_comb(k, _):
        comb_copy(k).wait_send()
        return 0

    lax.fori_loop(1, members, sent_comb, 0)
    for tile in weights:
        tile.sent()
    for i, (src, dst) in enumerate(stores):
        pltpu.make_async_copy(src, dst, store_sem.at[i]).wait()


def forward_call(
    grps, exps, lengths, bias_table, routes_t, tokens, cotangent, gains, router, qkv_t, out_w, in_low, down_slab
):
    reps = grps * QUAD
    rows, width = tokens.shape
    head_cols = width // exps
    row_block = qkv_t.shape[1]
    seg = math.gcd(qkv_t.shape[0], head_cols)
    segs = qkv_t.shape[0] // seg
    units = down_slab.shape[0]
    out_cols = out_w.shape[1]
    heads = HEADS // exps
    members = QUAD * exps
    tiles = Tiles(units, reps)
    shape = jax.ShapeDtypeStruct
    vmem = pl.BlockSpec(memory_space=pltpu.VMEM)
    smem = pl.BlockSpec(memory_space=pltpu.SMEM)
    hbm = pl.BlockSpec(memory_space=pl.ANY)
    results = [
        (shape((2, width, 2 * tiles.size), low), hbm),
        (shape((2, tiles.size, width), low), hbm),
        (shape((members, rows, width), low), hbm),
        (shape((members, rows, width), low), hbm),
        (shape((members, 8, rows), full), hbm),
        (shape((exps, rows, 3 * head_cols), low), hbm),
        (shape((exps, rows, 128), full), hbm),
        (shape((exps, rows, head_cols), low), hbm),
        (shape((exps, rows, width), low), hbm),
        (shape((exps, 3 * head_cols, row_block), low), hbm),
        (shape((exps, reps, row_block, out_cols), low), hbm),
        (shape((rows, width), full), vmem),
        (shape((rows, width), low), vmem),
        (shape((rows, 128), full), vmem),
    ]
    dma = pltpu.SemaphoreType.DMA
    chips = members // 2
    return pl.pallas_call(
        functools.partial(forward_kernel, grps, exps),
        out_shape=[r[0] for r in results],
        in_specs=[smem] * 2 + [vmem] * 7 + [hbm] * 2,
        out_specs=[r[1] for r in results],
        scratch_shapes=[
            pltpu.VMEM((exps, rows, width), low),
            pltpu.VMEM((exps, 3 * head_cols, row_block), low),
            pltpu.VMEM((exps, reps, row_block, out_cols), low),
            pltpu.VMEM((exps, rows, width), low),
            pltpu.VMEM((exps, rows, 3 * head_cols), low),
            pltpu.VMEM((exps, rows, 128), full),
            pltpu.VMEM((exps, rows, head_cols), low),
            pltpu.VMEM((exps, rows, head_cols), low),
            pltpu.VMEM((heads, rows, rows), full),
            pltpu.VMEM((8, rows), full),
            pltpu.VMEM((tiles.skip, width), low),
            dma((2, exps)),
            dma((2, max(segs * reps, exps * 3 * head_cols // seg))),
            dma((2, reps)),
            dma((2, exps)),
            dma((2, 2, 2 * reps)),
            dma((2, 2, reps + 1)),
            dma((2, exps)),
            dma((2, 3 * chips)),
            dma((2, 3 * chips + 1)),
            dma((2, 3 * chips)),
            dma((2, 3 * chips + 1)),
            dma((2, members)),
            dma((6,)),
        ],
        compiler_params=pltpu.CompilerParams(
            collective_id=0, has_side_effects=True, vmem_limit_bytes=60 * 1024 * 1024
        ),
        name="forward",
    )(lengths, bias_table, routes_t, tokens, cotangent, gains, router, qkv_t, out_w, in_low, down_slab)


def expert_kernel(
    grps,
    exps,
    cap,
    deal,
    routes_t,
    comb,
    n_all,
    cot_all,
    both_w,
    down_w,
    in_low,
    down_slab,
    n_sum,
    y_sum,
    c_sum,
    both_g,
    down_g,
    in_parts,
    down_parts,
    place,
    marks,
    n_rows,
    g_rows,
    both_v,
    down_v,
    raw_n,
    raw_g,
    y_acc,
    n_acc,
    both_d,
    active,
    both_stage,
    down_stage,
    out_n,
    out_y,
    load_sem,
    raw_sem,
    out_sem,
    in_sem,
    in_down_sem,
    home_sem,
    home_down_sem,
    stage_sem,
):
    at = Where(grps, exps)
    rows, width = n_all.shape[1:]
    tiles = Tiles(down_slab.shape[0], at.reps)
    size = tiles.size
    slots = exps * cap
    members = QUAD * exps
    loads = [pltpu.make_async_copy(both_w.at[t], both_v.at[t], load_sem.at[0, t]) for t in range(2)] + [
        pltpu.make_async_copy(down_w.at[t], down_v.at[t], load_sem.at[1, t]) for t in range(2)
    ]
    for copy in loads:
        copy.start()

    def raw_copies(q):
        here = pl.ds(pl.multiple_of(q * exps, exps), exps)
        return [
            pltpu.make_async_copy(n_all.at[here], raw_n.at[q % 2], raw_sem.at[0, q % 2]),
            pltpu.make_async_copy(cot_all.at[here], raw_g.at[q % 2], raw_sem.at[1, q % 2]),
        ]

    for copy in raw_copies(0):
        copy.start()
    greet_all(at)
    last = tiles.count - 1
    incoming = Outward(
        at, tiles, last, in_low, down_slab, both_v.at[last], down_v.at[last], None, in_sem, in_down_sem
    )
    incoming.start()
    home = Homeward(
        at, tiles, 0, both_stage.at[0], down_stage.at[0], in_parts, down_parts, home_sem, home_down_sem
    )

    earlier = jnp.where(row_of((rows, rows)) < lane_of((rows, rows)), 1.0, 0.0).astype(low)
    slot = row_of((cap, rows)).astype(full)

    def dispatch(q, _):
        @pl.when(q + 1 < QUAD)
        def _():
            for copy in raw_copies(q + 1):
                copy.start()

        for copy in raw_copies(q):
            copy.wait()
        lines = []
        for j in range(exps):
            seq = at.grp * members + q * exps + j
            pair = routes_t[:, pl.ds(pl.multiple_of(seq * rows, rows), rows)]
            lines.append(jnp.logical_or(pair[0:1] == at.exp, pair[1:2] == at.exp))
        lines = [jnp.where(line, 1.0, 0.0) for line in lines] + [jnp.zeros((8 - exps, rows), full)]
        hot_low = jnp.concatenate(lines, axis=0).astype(low)
        before = dot(hot_low, earlier)
        for j in range(exps):
            s = q * exps + j
            inside = jnp.logical_and(slot == before[j : j + 1, :], hot_low[j : j + 1, :].astype(full) > 0.5)
            here = jnp.where(inside, 1.0, 0.0)
            place[s] = here.astype(low)
            g = raw_g[q % 2, 0]
            for b in range(1, exps):
                g = jnp.where(deal[at.grp * members + s] == at.grp * members + q * exps + b, raw_g[q % 2, b], g)
            where = pl.ds(pl.multiple_of(s * cap, cap), cap)
            n_rows[where] = dot(here.astype(low), raw_n[q % 2, j]).astype(low)
            g_rows[where] = dot(here.astype(low), g).astype(low)
            marks[where, 0:1] = jnp.sum(here * comb[s, pl.ds(at.exp, 1), :], axis=1, keepdims=True)
            marks[where, 1:2] = jnp.zeros((cap, 1), full)
        return 0

    lax.fori_loop(0, QUAD, dispatch, 0)
    for copy in loads:
        copy.wait()
    curve = math.sqrt(2.0 / math.pi)

    def tile_work(f, _):
        @pl.when(f == last)
        def _():
            incoming.arrive()

        def chunk(c, _):
            here = pl.ds(pl.multiple_of(c * slots, slots), slots)
            share = marks[here, 0:1]
            both = dot(n_rows[here], both_v[f])
            gate_part, up_part = both[:, :size], both[:, size:]
            grad = nt(g_rows[here], down_v[f])
            square = gate_part * gate_part
            bend = jnp.tanh(curve * gate_part * (1.0 + 0.044715 * square))
            half = 0.5 * (1.0 + bend)
            gelu = gate_part * half
            slope = half + (0.5 * curve) * gate_part * (1.0 - bend * bend) * (1.0 + (3 * 0.044715) * square)
            value = gelu * up_part
            marks[here, 1:2] += jnp.sum(value * grad, axis=1, keepdims=True)
            grad = grad * share
            active[here] = (value * share).astype(low)
            both_d[here, :size] = (grad * up_part * slope).astype(low)
            both_d[here, size:] = (grad * gelu).astype(low)
            y = dot(active[here], down_v[f])
            y_acc[here] = jnp.where(f == 0, y, y_acc[here].astype(full) + y).astype(low)
            n_back = nt(both_d[here], both_v[f])
            n_acc[here] = jnp.where(f == 0, n_back, n_acc[here] + n_back)
            return 0

        lax.fori_loop(0, QUAD, chunk, 0)

        def columns(m, _):
            cols = pl.ds(pl.multiple_of(m * (width // 2), width // 2), width // 2)
            both_stage[f, cols] = tn(n_rows[:, cols], both_d[...]).astype(low)
            down_stage[f, :, cols] = tn(active[...], g_rows[:, cols]).astype(low)
            return 0

        lax.fori_loop(0, 2, columns, 0)

        @pl.when(f == 0)
        def _():
            home.start()

        @pl.when(f > 0)
        def _():
            for copy in stage_copies(f):
                copy.start()

        return 0

    def stage_copies(f):
        return [
            pltpu.make_async_copy(both_stage.at[f], both_g.at[f - 1], stage_sem.at[0, f]),
            pltpu.make_async_copy(down_stage.at[f], down_g.at[f - 1], stage_sem.at[1, f]),
        ]

    lax.fori_loop(0, tiles.count, tile_work, 0)

    def out_copies(s):
        return [
            pltpu.make_async_copy(out_n.at[s % 2], n_sum.at[s], out_sem.at[0, s % 2]),
            pltpu.make_async_copy(out_y.at[s % 2], y_sum.at[s], out_sem.at[1, s % 2]),
        ]

    def gather(s, _):
        @pl.when(s >= 2)
        def _():
            for copy in out_copies(s - 2):
                copy.wait()

        where = pl.ds(pl.multiple_of(s * cap, cap), cap)
        out_n[s % 2] = tn(place[s], n_acc[where].astype(low)).astype(low)
        out_y[s % 2] = tn(place[s], y_acc[where]).astype(low)
        line = jnp.sum(place[s].astype(full) * marks[where, 1:2], axis=0, keepdims=True)
        c_sum[s] = jnp.broadcast_to(line, (8, rows))
        for copy in out_copies(s):
            copy.start()
        return 0

    lax.fori_loop(0, members, gather, 0)
    for s in (members - 2, members - 1):
        for copy in out_copies(s):
            copy.wait()
    for f in range(1, tiles.count):
        for copy in stage_copies(f):
            copy.wait()
    home.arrive()
    incoming.sent()
    home.sent()


def expert_call(grps, exps, cap, deal, routes_t, comb_all, n_all, cot_all, both_w, down_w, in_low, down_slab):
    members, rows, width = n_all.shape
    reps = grps * QUAD
    tiles = Tiles(down_slab.shape[0], reps)
    size = tiles.size
    slab, both_hidden = in_low.shape
    units = down_slab.shape[0]
    slots = exps * cap
    shape = jax.ShapeDtypeStruct
    vmem = pl.BlockSpec(memory_space=pltpu.VMEM)
    smem = pl.BlockSpec(memory_space=pltpu.SMEM)
    hbm = pl.BlockSpec(memory_space=pl.ANY)
    results = [
        (shape((members, rows, width), low), hbm),
        (shape((members, rows, width), low), hbm),
        (shape((members, 8, rows), full), vmem),
        (shape((2, width, 2 * size), low), hbm),
        (shape((2, size, width), low), hbm),
        (shape((grps, slab, both_hidden), low), hbm),
        (shape((grps, units, width), low), hbm),
    ]
    dma = pltpu.SemaphoreType.DMA
    return pl.pallas_call(
        functools.partial(expert_kernel, grps, exps, cap),
        out_shape=[r[0] for r in results],
        in_specs=[smem] + [vmem] * 2 + [hbm] * 6,
        out_specs=[r[1] for r in results],
        scratch_shapes=[
            pltpu.VMEM((members, cap, rows), low),
            pltpu.VMEM((QUAD * slots, 128), full),
            pltpu.VMEM((QUAD * slots, width), low),
            pltpu.VMEM((QUAD * slots, width), low),
            pltpu.VMEM((tiles.count, width, 2 * size), low),
            pltpu.VMEM((tiles.count, size, width), low),
            pltpu.VMEM((2, exps, rows, width), low),
            pltpu.VMEM((2, exps, rows, width), low),
            pltpu.VMEM((QUAD * slots, width), low),
            pltpu.VMEM((QUAD * slots, width), full),
            pltpu.VMEM((QUAD * slots, 2 * size), low),
            pltpu.VMEM((QUAD * slots, size), low),
            pltpu.VMEM((tiles.count, width, 2 * size), low),
            pltpu.VMEM((tiles.count, size, width), low),
            pltpu.VMEM((2, rows, width), low),
            pltpu.VMEM((2, rows, width), low),
            dma((2, 2)),
            dma((2, 2)),
            dma((2, 2)),
            dma((2, 2 * reps)),
            dma((2, reps + 1)),
            dma((2, 2 * reps)),
            dma((2, max(QUAD, grps))),
            dma((2, tiles.count)),
        ],
        compiler_params=pltpu.CompilerParams(
            collective_id=2, has_side_effects=True, vmem_limit_bytes=60 * 1024 * 1024
        ),
        name="experts",
    )(deal, routes_t, comb_all, n_all, cot_all, both_w, down_w, in_low, down_slab)


def adam_kernel(exps, *refs):
    in_parts, down_parts, qkv_grad, out_grad, small = refs[:5]
    states, news, bias_grad = refs[5:26], refs[26:47], refs[47]
    heads = HEADS // exps
    width = small.shape[1]

    def update(i, grad, rate, decay):
        weight, first, second = [state[...] for state in states[3 * i : 3 * i + 3]]
        values = adamw_update(weight, first, second, grad, rate, decay)
        for new, value in zip(news[3 * i : 3 * i + 3], values, strict=True):
            new[...] = value

    def total(parts):
        result = parts[0].astype(full)
        for k in range(1, parts.shape[0]):
            result = result + parts[k].astype(full)
        return result

    @pl.when(pl.program_id(0) == 0)
    def _():
        update(0, qkv_grad[...], 1.5 / math.sqrt(D), 0.1)
        update(1, out_grad[...], 6.0 / math.sqrt(D), 0.1)
        for e in range(exps):
            for h in range(heads):
                bias_grad[e * heads + h : e * heads + h + 1, :] = small[
                    exps + 3 + e : exps + 4 + e, h * 128 : h * 128 + BUCKETS
                ]
        update(2, bias_grad[...], 0.3, 0.0)
        update(3, small[0:exps, :], 1.0 / math.sqrt(D), 0.1)
        update(4, small[exps : exps + 2, :], 0.5, 0.0)

    update(5, total(in_parts), 1.5 / math.sqrt(D), 0.1)
    update(6, total(down_parts), 1.5 / math.sqrt(FF), 0.1)


def adam_call(exps, in_parts, down_parts, qkv_grad, out_grad, small, states):
    steps = 4

    def whole(array):
        return pl.BlockSpec(array.shape, lambda i: (0,) * array.ndim)

    def columns(array):
        block = array.shape[:-1] + (array.shape[-1] // steps,)
        return pl.BlockSpec(block, lambda i: (0,) * (array.ndim - 1) + (i,))

    specs = [whole(state) for state in states[:15]] + [columns(state) for state in states[15:]]
    return pl.pallas_call(
        functools.partial(adam_kernel, exps),
        grid=(steps,),
        in_specs=[columns(in_parts), columns(down_parts), whole(qkv_grad), whole(out_grad), whole(small)] + specs,
        out_specs=specs,
        out_shape=[jax.ShapeDtypeStruct(state.shape, full) for state in states],
        scratch_shapes=[pltpu.VMEM((HEADS, BUCKETS), full)],
        compiler_params=pltpu.CompilerParams(vmem_limit_bytes=60 * 1024 * 1024),
        name="adam",
    )(in_parts, down_parts, qkv_grad, out_grad, small, *states)


class Halving:
    def __init__(self, at, source, kept, bufs, sems, load_sem, orders):
        self.at, self.source, self.kept, self.bufs = at, source, kept, bufs
        self.sems, self.load_sem = sems, load_sem
        self.plane = at.quad * at.exps + at.exp
        self.places = bits_of(QUAD * at.exps)
        self.chip_bits = list(range(self.places - 1))
        self.parts = column_parts(source.shape[2])
        self.orders = orders

    def device(self, bit):
        other = flipped(self.plane, bit)
        return (self.at.grp, other // self.at.exps, other % self.at.exps)

    def first(self):
        core = self.plane % 2
        count = 1 << (self.places - 1)
        device = self.device(0)

        def copies(j):
            return send(
                self.source.at[2 * j + 1 - core], self.bufs[0].at[j], self.sems.at[0, 0, j], self.sems.at[0, 1, j], device
            )

        def load(j):
            return pltpu.make_async_copy(self.source.at[2 * j + core], self.kept.at[j], self.load_sem.at[j])

        return count, copies, load

    def start_first(self):
        count, copies, load = self.first()

        def one(j, _):
            copies(j).start()
            load(j).start()
            return 0

        lax.fori_loop(0, count, one, 0)

    def add_first(self):
        count, copies, load = self.first()

        def one(j, _):
            arrived(self.bufs[0].at[j], self.sems.at[0, 1, j])
            load(j).wait()
            self.bufs[0][j] = (self.bufs[0][j].astype(full) + self.kept[j].astype(full)).astype(low)
            return 0

        lax.fori_loop(0, count, one, 0)

    def hop(self, step, part):
        order = self.orders[part]
        bit = order[step]
        left = [b for b in self.chip_bits if b not in order[:step]]
        pos = left.index(bit)
        half = 1 << (len(left) - 1)
        mine = (self.plane // (1 << (bit + 1))) % 2
        device = self.device(bit + 1)
        begin, size = self.parts[part]
        cols = pl.ds(begin, size)
        base = self.base(step, part)

        def index(j, value):
            return (j >> pos) * (1 << (pos + 1)) + value * (1 << pos) + j % (1 << pos)

        pairs = []
        for j in range(half):
            copy = functools.partial(
                send,
                self.bufs[step].at[index(j, 1 - mine), :, cols],
                self.bufs[step + 1].at[j, :, cols],
                self.sems.at[1, 0, base + j],
                self.sems.at[1, 1, base + j],
                device,
            )
            pairs.append((copy, index(j, mine), j))
        return pairs, begin, size, base

    def base(self, step, part):
        n = len(self.chip_bits)
        return part * (1 << n) + sum(1 << (n - 1 - s) for s in range(step))

    def start(self, step, part=None):
        for p in range(3) if part is None else [part]:
            for copy, _, _ in self.hop(step, p)[0]:
                copy().start()

    def add(self, step, part):
        pairs, begin, size, base = self.hop(step, part)
        cols = pl.ds(begin, size)
        here, there = self.bufs[step], self.bufs[step + 1]
        for _, keep, j in pairs:
            arrived(there.at[j, :, cols], self.sems.at[1, 1, base + j])
            there[j, :, begin : begin + size] = (
                there[j, :, begin : begin + size].astype(full) + here[keep, :, begin : begin + size].astype(full)
            ).astype(low)

    def next(self, step):
        for p in range(3):
            self.add(step, p)
            if step + 1 < len(self.chip_bits):
                self.start(step + 1, p)

    def result(self):
        return self.bufs[len(self.chip_bits)]

    def finish(self):
        count, copies, _ = self.first()

        def one(j, _):
            copies(j).wait_send()
            return 0

        lax.fori_loop(0, count, one, 0)
        for step in range(len(self.chip_bits)):
            for p in range(3):
                for copy, _, _ in self.hop(step, p)[0]:
                    copy().wait_send()


def backward_kernel(
    grps,
    exps,
    lengths,
    deal,
    bias_table,
    n_parts,
    y_parts,
    c_parts,
    both_g,
    down_g,
    in_before,
    down_before,
    n1_in,
    cot_all,
    routes_t,
    tokens,
    h1_in,
    n2_in,
    probs_in,
    qkv,
    lse,
    mine,
    wqkv,
    wout,
    gains,
    router_t,
    *rest,
):
    token_grad, block_out, in_parts, down_parts, qkv_grad, out_grad, small_out = rest[:7]
    scratch = rest[7:]
    (
    kept,
    n_bufs,
    y_bufs,
    c_in,
    dh1,
    dz_send,
    dz_all,
    do_send,
    do_in,
    bias,
    bias_sum,
    dqkv,
    dqkv_t,
    dn1_send,
    dn1_in,
    wq_send,
    og_send,
    qkv_parts,
    out_parts,
    blk_send,
    blk_in,
    small_send,
    small_exp,
    small_sum,
    small_rep,
    n_sem,
    y_sem,
    load_sem,
    c_sem,
    weight_sem,
    down_sem,
    dz_sem,
    do_sem,
    dn1_sem,
    wq_sem,
    og_sem,
    blk_sem,
    small_sem,
    small2_sem,
    n1_sem,
    ) = scratch
    at = Where(grps, exps)
    reps = at.reps
    rows, width = tokens.shape
    heads = HEADS // exps
    head_dim = width // HEADS
    head_cols = heads * head_dim
    block_cols = min(128, head_cols)
    row_block = wqkv.shape[2]
    out_cols = wout.shape[3]
    tiles = Tiles(down_parts.shape[1], reps)
    scale = 1.0 / math.sqrt(head_dim)
    SEND, RECV = 0, 1
    plane = at.quad * exps + at.exp
    members = QUAD * exps

    def exp_peer(k):
        return (at.exp + k) % exps

    router = router_t[...]
    n1 = kept.at[0:exps]
    group = pl.ds(pl.multiple_of(at.quad * exps, exps), exps)
    cot_copy = pltpu.make_async_copy(cot_all.at[group], dn1_send, n1_sem.at[1])
    cot_copy.start()
    greet_all(at)

    dn = Halving(at, n_parts, kept, n_bufs, n_sem, load_sem.at[0], [[0, 1, 2], [1, 2, 0], [2, 0, 1]])
    ys = Halving(at, y_parts, kept, y_bufs, y_sem, load_sem.at[1], [[1, 0, 2], [1, 0, 2], [0, 1, 2]])
    dn.start_first()
    homes = [
        Homeward(
            at, tiles, t + 1, both_g.at[t], down_g.at[t], in_parts, down_parts, weight_sem.at[t], down_sem.at[t]
        )
        for t in range(2)
    ]
    homes[0].start()
    n1_copy = pltpu.make_async_copy(n1_in, n1, n1_sem.at[0])

    def c_copy(k):
        other = (plane + k) % members
        return other, send(
            c_parts.at[other],
            c_in.at[plane],
            c_sem.at[SEND, other],
            c_sem.at[RECV, plane],
            (at.grp, other // exps, other % exps),
        )

    def start_c(k, _):
        c_copy(k)[1].start()
        return 0

    lax.fori_loop(1, members, start_c, 0)
    pltpu.make_async_copy(c_parts.at[plane], c_in.at[plane], c_sem.at[RECV, plane]).start()

    span = 2 * rows
    bucket = bucket_of(lane_of((8, span)) - rows)
    for h in range(heads):
        line = jnp.zeros((8, span), full)
        for b in range(BUCKETS):
            line = jnp.where(bucket == b, bias_table[at.exp * heads + h, b], line)
        whole = jnp.broadcast_to(line[0:1], (rows, span))
        bias[h] = pltpu.roll(whole, 0, 1, stride=1, stride_axis=0)[:, rows:]

    dn.add_first()
    dn.start(0)
    ys.start_first()

    def wait_c(k, _):
        arrived(c_in.at[k], c_sem.at[RECV, k])
        return 0

    lax.fori_loop(0, members, wait_c, 0)
    lane = lane_of((rows, 128))
    comb_rows = []
    for e in range(exps):
        total = c_in[e]
        for q in range(1, QUAD):
            total = total + c_in[q * exps + e]
        comb_rows.append(total[0:1, :])
    comb_rows.append(jnp.zeros((128 - exps, rows), full))
    comb_grad = jnp.concatenate(comb_rows, axis=0).T
    valid = row_of((rows, 1)) < lengths[at.me]
    probs = probs_in[...]
    hot = routed(routes_t, at.me, rows)
    picked = jnp.where(hot, probs, 0.0)
    total = jnp.sum(picked, axis=1, keepdims=True)
    gate = picked / total
    gate_grad_rows = jnp.where(valid, comb_grad, 0.0)
    spread_grad = jnp.sum(gate_grad_rows * gate, axis=1, keepdims=True)
    probs_grad = jnp.where(hot, (gate_grad_rows - spread_grad) / total, 0.0)
    logit_grad = probs * (probs_grad - jnp.sum(probs_grad * probs, axis=1, keepdims=True))
    n2 = n2_in[...].astype(full)
    router_rows = lax.dot_general(
        logit_grad, n2, (((0,), (0,)), ((), ())), preferred_element_type=full, precision=highest
    )
    small_rows = small_send.shape[0]
    small_send[...] = jnp.zeros_like(small_send)
    small_send[0:exps, :] = router_rows[0:exps, :]
    router_back = jnp.dot(
        logit_grad, jnp.concatenate([router, jnp.zeros((128 - exps, width), full)], axis=0),
        precision=highest, preferred_element_type=full,
    )
    h1 = h1_in[...]
    r2 = lax.rsqrt(jnp.mean(h1 * h1, axis=1, keepdims=True) + eps_norm)

    dn.next(0)
    ys.add_first()
    n1_copy.start()
    dn.next(1)
    steps = len(dn.chip_bits)
    for step in range(2, steps):
        dn.next(step)

    n2_grad = router_back + dn.result()[0].astype(full)
    scaled = n2_grad * gains[1:2, :]
    cot_copy.wait()
    dealt = deal[at.me] - at.base
    g = dn1_send[0]
    for e in range(1, exps):
        g = jnp.where(dealt == e, dn1_send[e], g)
    hidden_grad = (
        jnp.where(valid, g.astype(full), 0.0)
        + r2 * scaled
        - h1 * (r2 * r2 * r2) * jnp.mean(scaled * h1, axis=1, keepdims=True)
    )
    dh1[...] = hidden_grad
    small_send[exps + 1 : exps + 2, :] = jnp.sum(n2_grad * h1 * r2, axis=0, keepdims=True)
    branch = hidden_grad.astype(low)
    dz_send[...] = branch
    for e in range(exps):
        total = jnp.zeros((rows, row_block), full)
        for r in range(reps):
            total = total + nt(branch[:, r * out_cols : (r + 1) * out_cols], wout[e, r])
        do_send[e] = total.astype(low)

    def do_copies():
        return [
            send(
                do_send.at[exp_peer(k)],
                do_in.at[at.exp],
                do_sem.at[SEND, exp_peer(k)],
                do_sem.at[RECV, at.exp],
                at.device(at.rep, exp_peer(k)),
            )
            for k in range(1, exps)
        ]

    for copy in do_copies():
        copy.start()
    pltpu.make_async_copy(do_send.at[at.exp], do_in.at[at.exp], do_sem.at[RECV, at.exp]).start()

    group_dz = Group(at, dz_send, dz_all, dz_sem)
    group_dz.start()
    dz_all[at.exp] = branch
    homes[1].start()
    ys.start(0)

    bias_sum[...] = jnp.zeros_like(bias_sum)

    def og_copies():
        return [
            send(
                og_send.at[(at.rep + k) % reps],
                out_parts.at[at.rep],
                og_sem.at[SEND, (at.rep + k) % reps],
                og_sem.at[RECV, at.rep],
                at.device((at.rep + k) % reps, at.exp),
            )
            for k in range(1, reps)
        ]

    group_blk = Group(at, blk_send, blk_in, blk_sem)

    def beside(k):
        if k == 1:
            group_dz.pass_on()
            return
        ys.next(k - 2)
        if k < exps - 1:
            return
        group_dz.arrive()
        grad = tn(mine[...].reshape(exps * rows, head_cols), dz_all[...].reshape(exps * rows, width))
        for r in range(reps):
            og_send[r] = grad[:, r * out_cols : (r + 1) * out_cols].astype(low)
        for copy in og_copies():
            copy.start()
        pltpu.make_async_copy(og_send.at[at.rep], out_parts.at[at.rep], og_sem.at[RECV, at.rep]).start()

    def dn1_copies():
        beside, across = turn(at.exp, 2), turn(at.exp, 1)
        return [
            functools.partial(
                send, dn1_send.at[k], dn1_in.at[j], dn1_sem.at[SEND, j], dn1_sem.at[RECV, j], at.device(at.rep, to)
            )
            for k, j, to in ((turn(at.exp, 0), 2, beside), (across, 0, across), (beside, 1, beside))
        ]

    def attend_back(i, _):
        s = turn(at.exp, i)
        for k in range(1, exps):

            @pl.when(i == k)
            def _():
                beside(k)

        arrived(do_in.at[s], do_sem.at[RECV, s])
        ok = lane_of((rows, rows)) < lengths[at.base + s]
        block_lane = lane_of((rows, block_cols))
        for c in range(head_cols // block_cols):
            cols = slice(c * block_cols, (c + 1) * block_cols)
            k_cols = slice(head_cols + c * block_cols, head_cols + (c + 1) * block_cols)
            v_cols = slice(2 * head_cols + c * block_cols, 2 * head_cols + (c + 1) * block_cols)
            q = qkv[s, :, cols]
            k = qkv[s, :, k_cols]
            v = qkv[s, :, v_cols]
            do = do_in[s, :, cols]
            dq = jnp.zeros((rows, block_cols), full)
            dk = jnp.zeros((rows, block_cols), full)
            dv = jnp.zeros((rows, block_cols), full)
            for t in range(block_cols // head_dim):
                h = c * (block_cols // head_dim) + t
                here = jnp.logical_and(block_lane >= t * head_dim, block_lane < (t + 1) * head_dim)
                zero = jnp.zeros_like(q)
                q_h = jnp.where(here, q, zero)
                do_h = jnp.where(here, do, zero)
                scores = nt(q_h, k) * scale + bias[h]
                total = jnp.sum(jnp.where(lane == h, lse[s], 0.0), axis=1, keepdims=True)
                p = jnp.where(ok, jnp.exp(scores - total), 0.0)
                dp = nt(do_h, v)
                delta = jnp.sum(dp * p, axis=1, keepdims=True)
                ds = (p * (dp - delta)).astype(low)
                bias_sum[h] += ds.astype(full)
                dv = jnp.where(here, tn(p.astype(low), do), dv)
                dq = jnp.where(here, jnp.dot(ds, k, preferred_element_type=full), dq)
                dk = jnp.where(here, tn(ds, q), dk)
            dqkv[:, cols] = (dq * scale).astype(low)
            dqkv[:, k_cols] = (dk * scale).astype(low)
            dqkv[:, v_cols] = dv.astype(low)
        dqkv_t[:, pl.ds(pl.multiple_of(s * rows, rows), rows)] = dqkv[...].T
        for e in range(exps):
            dn1_send[s, :, e * row_block : (e + 1) * row_block] = jnp.dot(
                dqkv[...], wqkv[e], preferred_element_type=full
            ).astype(low)

        @pl.when(i == 0)
        def _():
            dn1_copies()[0]().start()

        @pl.when(i == 1)
        def _():
            arrived(dn1_in.at[2], dn1_sem.at[RECV, 2])
            dn1_send[s] = (dn1_send[s].astype(full) + dn1_in[2].astype(full)).astype(low)
            dn1_copies()[1]().start()

        @pl.when(i == 2)
        def _():
            dn1_copies()[2]().start()

        return 0

    lax.fori_loop(0, exps, attend_back, 0)

    n1_copy.wait()
    seg = wq_send.shape[2]
    segs = qkv_parts.shape[1]
    parts = wq_send.shape[1]
    for e in range(exps):
        part = kept[0:exps, :, e * row_block : (e + 1) * row_block].reshape(exps * rows, row_block)
        total = dot(dqkv_t[...], part)
        for j in range(parts):
            wq_send[e, j] = total[j * seg : (j + 1) * seg].astype(low)

    def owner(j):
        section, within = j // (head_cols // seg), j % (head_cols // seg)
        col = section * width + at.exp * head_cols + within * seg
        block = col // seg
        return block // segs, block % segs

    def wq_copy(i):
        e, j = i // parts, i % parts
        rep, k = owner(j)
        dst = qkv_parts.at[at.rep, k]
        recv = wq_sem.at[RECV, at.rep * segs + k]
        stays = jnp.logical_and(rep == at.rep, e == at.exp)
        return (
            stays,
            functools.partial(send, wq_send.at[e, j], dst, wq_sem.at[SEND, i], recv, at.device(rep, e)),
            functools.partial(pltpu.make_async_copy, wq_send.at[e, j], dst, recv),
        )

    def start_wq(i, _):
        stays, away, local = wq_copy(i)

        @pl.when(stays)
        def _():
            local().start()

        @pl.when(jnp.logical_not(stays))
        def _():
            away().start()

        return 0

    lax.fori_loop(0, exps * parts, start_wq, 0)
    n1_grad = dn1_send[at.exp].astype(full)
    for j in range(2):
        arrived(dn1_in.at[j], dn1_sem.at[RECV, j])
        n1_grad = n1_grad + dn1_in[j].astype(full)
    x = tokens[...].astype(full)
    r1 = lax.rsqrt(jnp.mean(x * x, axis=1, keepdims=True) + eps_norm)
    scaled = n1_grad * gains[0:1, :]
    token_grad[...] = (
        dh1[...] + r1 * scaled - x * (r1 * r1 * r1) * jnp.mean(scaled * x, axis=1, keepdims=True)
    )
    small_send[exps : exps + 1, :] = jnp.sum(n1_grad * x * r1, axis=0, keepdims=True)

    line_lane = lane_of((8, 128))
    line_row = row_of((8, 128))
    bias_line = jnp.zeros((8, 128), full)
    flip = jnp.where(row_of((rows, rows)) + lane_of((rows, rows)) == rows - 1, 1.0, 0.0).astype(low)
    turned_bucket = bucket_of(rows - 1 - lane_of((8, span)))
    for h in range(heads):
        high = bias_sum[h].astype(low)
        rest = (bias_sum[h] - high.astype(full)).astype(low)
        flipped = dot(high, flip) + dot(rest, flip)
        square = jnp.concatenate([flipped, jnp.zeros((rows, rows), full)], axis=1)
        turned = pltpu.roll(square, 0, 1, stride=1, stride_axis=0)
        sums = jnp.broadcast_to(jnp.sum(turned, axis=0, keepdims=True), (8, span))
        for b in range(BUCKETS):
            value = jnp.sum(jnp.where(turned_bucket == b, sums, 0.0), axis=1, keepdims=True)
            bias_line = jnp.where(jnp.logical_and(line_row == h, line_lane == b), value, bias_line)
    for h in range(heads):
        small_send[exps + 2 : exps + 3, h * 128 : (h + 1) * 128] = bias_line[h : h + 1, :]

    for step in range(exps - 2, steps):
        ys.next(step)
    block = jnp.where(valid, h1_in[...] + ys.result()[0].astype(full), 0.0).astype(low)
    blk_send[...] = block
    group_blk.start()
    blk_in[at.exp] = block

    def small_copies():
        return [
            send(
                small_send,
                small_exp.at[at.exp],
                small_sem.at[SEND, exp_peer(k)],
                small_sem.at[RECV, at.exp],
                at.device(at.rep, exp_peer(k)),
            )
            for k in range(1, exps)
        ]

    for copy in small_copies():
        copy.start()
    small_exp[at.exp] = small_send[...]
    for k in range(1, exps):
        arrived(small_exp.at[exp_peer(k)], small_sem.at[RECV, exp_peer(k)])
    total = small_exp[0]
    for e in range(1, exps):
        total = total + small_exp[e]
    small_sum[0] = total
    for e in range(exps):
        small_sum[0, exps + 3 + e : exps + 4 + e, :] = small_exp[e, exps + 2 : exps + 3, :]

    def small2_copies():
        return [
            send(
                small_sum.at[0],
                small_rep.at[at.rep],
                small2_sem.at[SEND, (at.rep + k) % reps],
                small2_sem.at[RECV, at.rep],
                at.device((at.rep + k) % reps, at.exp),
            )
            for k in range(1, reps)
        ]

    for copy in small2_copies():
        copy.start()
    small_rep[at.rep] = small_sum[0]
    group_blk.pass_on()
    group_blk.arrive()
    chosen = jnp.zeros((rows, width), full)
    for e in range(exps):
        chosen = jnp.where(deal[at.base + e] == at.me, blk_in[e].astype(full), chosen)
    block_out[...] = chosen.astype(low)
    for k in range(1, reps):
        arrived(small_rep.at[(at.rep + k) % reps], small2_sem.at[RECV, (at.rep + k) % reps])
    total = small_rep[0]
    for r in range(1, reps):
        total = total + small_rep[r]
    small_out[...] = total

    for r in range(reps):
        arrived(out_parts.at[r], og_sem.at[RECV, r])
    grad = out_parts[0].astype(full)
    for r in range(1, reps):
        grad = grad + out_parts[r].astype(full)
    out_grad[...] = grad

    def wq_in(i, _):
        arrived(qkv_parts.at[i // segs, i % segs], wq_sem.at[RECV, i])
        return 0

    lax.fori_loop(0, reps * segs, wq_in, 0)
    grads = []
    for k in range(segs):
        grad = qkv_parts[0, k].astype(full)
        for r in range(1, reps):
            grad = grad + qkv_parts[r, k].astype(full)
        grads.append(grad.T)
    qkv_grad[...] = jnp.concatenate(grads, axis=1)
    for home in homes:
        home.arrive()

    def sent_c(k, _):
        c_copy(k)[1].wait_send()
        return 0

    lax.fori_loop(1, members, sent_c, 0)
    dn.finish()
    ys.finish()

    for home in homes:
        home.sent()

    def sent_wq(i, _):
        stays, away, _ = wq_copy(i)

        @pl.when(jnp.logical_not(stays))
        def _():
            away().wait_send()

        return 0

    lax.fori_loop(0, exps * parts, sent_wq, 0)
    for copies in (do_copies(), og_copies(), small_copies(), small2_copies()):
        for copy in copies:
            copy.wait_send()
    for copy in dn1_copies():
        copy().wait_send()
    group_dz.sent()
    group_blk.sent()


def routed(routes_t, seq, rows):
    pair = routes_t[:, pl.ds(pl.multiple_of(seq * rows, rows), rows)].astype(full)
    cols = jnp.concatenate([pair, jnp.zeros((126, rows), full)], axis=0).T
    lane = lane_of((rows, 128)).astype(full)
    return jnp.logical_or(lane == cols[:, 0:1], lane == cols[:, 1:2])


def backward_call(
    grps, exps, lengths, deal, bias_table, n_parts, y_parts, c_parts, both_g, down_g, in_before, down_before, n1,
    cot_all, routes_t, tokens, h1, n2, probs, qkv, lse, mine, wqkv, wout, gains, router
):
    reps = grps * QUAD
    rows, width = tokens.shape
    heads = HEADS // exps
    head_cols = width // exps
    row_block = wqkv.shape[2]
    out_cols = wout.shape[3]
    shard_cols = 3 * width // reps
    seg = math.gcd(shard_cols, head_cols)
    segs = shard_cols // seg
    parts = 3 * head_cols // seg
    members = QUAD * exps
    chip_bits = bits_of(members) - 1
    small_rows = -(-(2 * exps + 3) // 8) * 8
    shape = jax.ShapeDtypeStruct
    vmem = pl.BlockSpec(memory_space=pltpu.VMEM)
    smem = pl.BlockSpec(memory_space=pltpu.SMEM)
    hbm = pl.BlockSpec(memory_space=pl.ANY)
    results = [
        (shape((rows, width), full), vmem),
        (shape((rows, width), low), vmem),
        (shape(in_before.shape, low), hbm),
        (shape(down_before.shape, low), hbm),
        (shape((row_block, shard_cols), full), vmem),
        (shape((row_block, out_cols), full), vmem),
        (shape((small_rows, width), full), vmem),
    ]
    dma = pltpu.SemaphoreType.DMA
    bufs = [pltpu.VMEM((1 << (chip_bits - s), rows, width), low) for s in range(chip_bits + 1)]
    return pl.pallas_call(
        functools.partial(backward_kernel, grps, exps),
        out_shape=[r[0] for r in results],
        in_specs=[smem] * 3 + [hbm] * 9 + [vmem] * 12,
        out_specs=[r[1] for r in results],
        scratch_shapes=[
            pltpu.VMEM((members // 2, rows, width), low),
            list(bufs),
            list(bufs),
            pltpu.VMEM((members, 8, rows), full),
            pltpu.VMEM((rows, width), full),
            pltpu.VMEM((rows, width), low),
            pltpu.VMEM((exps, rows, width), low),
            pltpu.VMEM((exps, rows, head_cols), low),
            pltpu.VMEM((exps, rows, head_cols), low),
            pltpu.VMEM((heads, rows, rows), full),
            pltpu.VMEM((heads, rows, rows), full),
            pltpu.VMEM((rows, 3 * head_cols), low),
            pltpu.VMEM((3 * head_cols, exps * rows), low),
            pltpu.VMEM((exps, rows, width), low),
            pltpu.VMEM((3, rows, width), low),
            pltpu.VMEM((exps, parts, seg, row_block), low),
            pltpu.VMEM((reps, row_block, out_cols), low),
            pltpu.VMEM((reps, segs, seg, row_block), low),
            pltpu.VMEM((reps, row_block, out_cols), low),
            pltpu.VMEM((rows, width), low),
            pltpu.VMEM((exps, rows, width), low),
            pltpu.VMEM((small_rows, width), full),
            pltpu.VMEM((exps, small_rows, width), full),
            pltpu.VMEM((1, small_rows, width), full),
            pltpu.VMEM((reps, small_rows, width), full),
            dma((2, 2, 3 << chip_bits)),
            dma((2, 2, 3 << chip_bits)),
            dma((2, members // 2)),
            dma((2, members)),
            dma((2, 2, 2 * reps)),
            dma((2, 2, max(QUAD, grps))),
            dma((2, exps)),
            dma((2, exps)),
            dma((2, exps)),
            dma((2, max(exps * parts, reps * segs))),
            dma((2, reps)),
            dma((2, exps)),
            dma((2, exps)),
            dma((2, reps)),
            dma((2,)),
        ],
        compiler_params=pltpu.CompilerParams(
            collective_id=1, has_side_effects=True, vmem_limit_bytes=60 * 1024 * 1024
        ),
        input_output_aliases={8: 2, 9: 3},
        name="backward",
    )(
        lengths, deal, bias_table, n_parts, y_parts, c_parts, both_g, down_g, in_before, down_before, n1, cot_all,
        routes_t, tokens, h1, n2, probs, qkv, lse, mine, wqkv, wout, gains, router
    )


def per_device(
    tokens,
    cotangent,
    seq_lengths,
    deal,
    routes,
    attn_qkv,
    qkv_first,
    qkv_second,
    attn_out,
    out_first,
    out_second,
    rel_bias,
    bias_first,
    bias_second,
    router,
    router_first,
    router_second,
    norm_gains,
    gains_first,
    gains_second,
    expert_in,
    in_first,
    in_second,
    expert_out,
    down_first,
    down_second,
):
    rows, width = tokens.shape
    experts = router.shape[1]
    capacity = (10 * rows + 4 * experts - 1) // (4 * experts)
    exps = lax.axis_size("exp")
    grps = lax.axis_size("grp")
    in_low = expert_in[0].astype(low)
    down_low = expert_out[0].astype(low)
    routes_t = routes.T
    bias_table = rel_bias.T
    (
        both_w, down_w, cot_all, n_all, comb_all, qkv, lse, context_mine, normed_group, wqkv, wout, hidden_one,
        normed_two, router_probs,
    ) = forward_call(
        grps, exps, seq_lengths, bias_table, routes_t, tokens, cotangent, norm_gains.T, router.T,
        attn_qkv.astype(low).T, attn_out.astype(low), in_low, down_low,
    )
    n_parts, y_parts, c_parts, both_g, down_g, in_before, down_before = expert_call(
        grps, exps, capacity, deal, routes_t, comb_all, n_all, cot_all, both_w, down_w, in_low, down_low
    )
    token_grad, block_out, in_parts, down_parts, qkv_grad, out_grad, small = backward_call(
        grps, exps, seq_lengths, deal, bias_table, n_parts, y_parts, c_parts, both_g, down_g, in_before, down_before,
        normed_group, cot_all, routes_t, tokens, hidden_one, normed_two, router_probs, qkv, lse, context_mine, wqkv,
        wout, norm_gains.T, router.T,
    )
    states = [
        attn_qkv, qkv_first, qkv_second, attn_out, out_first, out_second, bias_table, bias_first.T, bias_second.T,
        router.T, router_first.T, router_second.T, norm_gains.T, gains_first.T, gains_second.T,
        expert_in[0], in_first[0], in_second[0], expert_out[0], down_first[0], down_second[0],
    ]
    new = list(adam_call(exps, in_parts, down_parts, qkv_grad, out_grad, small, states))
    new = new[:6] + [array.T for array in new[6:15]] + [array[None] for array in new[15:]]
    return (block_out, token_grad, *new)


def bucket_onehot(length):
    places = jnp.arange(length, dtype=jnp.int32)
    offset = places[None, :] - places[:, None]
    distance = jnp.abs(offset)
    bucket = 16 * (offset > 0).astype(jnp.int32)
    for threshold in thresholds:
        bucket = bucket + (distance >= threshold).astype(jnp.int32)
    return (bucket[:, :, None] == jnp.arange(BUCKETS, dtype=jnp.int32)[None, None, :]).astype(full)


def swap(pieces, axes):
    return lax.all_to_all(pieces, axes, split_axis=0, concat_axis=0, tiled=True)


def spread(block, axes):
    members = lax.axis_size(axes)
    return swap(jnp.broadcast_to(block[None], (members,) + block.shape), axes)


def plain_device(
    tokens,
    cotangent,
    seq_lengths,
    deal,
    routes,
    attn_qkv,
    qkv_first,
    qkv_second,
    attn_out,
    out_first,
    out_second,
    rel_bias,
    bias_first,
    bias_second,
    router,
    router_first,
    router_second,
    norm_gains,
    gains_first,
    gains_second,
    expert_in,
    in_first,
    in_second,
    expert_out,
    down_first,
    down_second,
):
    rows, width = tokens.shape
    head_dim = width // HEADS
    score_scale = 1.0 / math.sqrt(head_dim)
    experts = router.shape[1]
    capacity = (10 * rows + 4 * experts - 1) // (4 * experts)
    exps = lax.axis_size("exp")
    grps = lax.axis_size("grp")
    reps = grps * QUAD
    heads = HEADS // exps
    head_cols = heads * head_dim
    place = lax.axis_index("exp")
    base = lax.axis_index(REP) * exps
    me = base + place
    slab = expert_in.shape[1]
    units = expert_out.shape[1]
    quarter = grps * units

    row_block = attn_qkv.shape[0]
    qkv_rows = lax.all_gather(attn_qkv.astype(low), REP, axis=1, tiled=True)
    out_rows = lax.all_gather(attn_out.astype(low), REP, axis=1, tiled=True)
    qkv_pieces = jnp.transpose(
        qkv_rows.reshape(row_block, 3, exps, head_cols), (2, 0, 1, 3)
    ).reshape(exps, row_block, 3 * head_cols)
    qkv_mine = swap(qkv_pieces, "exp").reshape(width, 3 * head_cols)
    full_out = spread(out_rows, "exp").reshape(width, width)

    group_tokens = spread(tokens, "exp")
    group_cotangent = spread(cotangent, "exp")
    my_cotangent = lax.dynamic_index_in_dim(group_cotangent, deal[me] - base, 0, keepdims=False)

    my_routes = lax.dynamic_slice_in_dim(routes, me * rows, rows, 0)
    places = jnp.arange(rows, dtype=jnp.int32)
    valid_rows = (places < seq_lengths[me]).astype(full)
    group_lengths = lax.dynamic_slice_in_dim(seq_lengths, base, exps, 0)
    key_ok = places[None, :] < group_lengths[:, None]
    gain_one = norm_gains[:, 0]
    gain_two = norm_gains[:, 1]

    chosen = (my_routes[:, :, None] == jnp.arange(experts, dtype=jnp.int32)[None, None, :]).astype(full)
    flat_routes = my_routes.reshape(-1)
    route_hot = (flat_routes[:, None] == jnp.arange(experts, dtype=jnp.int32)[None, :]).astype(jnp.int32)
    before = jnp.cumsum(route_hot, axis=0) - route_hot
    slot_index = jnp.sum(before * route_hot, axis=-1)
    target = (flat_routes * capacity + slot_index).reshape(rows, 2)
    slots = experts * capacity
    slot_ids = jnp.arange(slots, dtype=jnp.int32)
    place_first = slot_ids[:, None] == target[None, :, 0]
    place_second = slot_ids[:, None] == target[None, :, 1]
    place_any = jnp.logical_or(place_first, place_second).astype(low)

    shard_in = expert_in[0].astype(low).reshape(slab, 2, grps, QUAD, units)
    in_pieces = jnp.transpose(shard_in, (1, 3, 0, 2, 4)).reshape(2, 1, QUAD, slab, quarter)
    in_pieces = jnp.broadcast_to(in_pieces, (2, grps, QUAD, slab, quarter)).reshape(
        2, reps, slab, quarter
    )
    down_mine = spread(expert_out[0].astype(low), "grp").reshape(quarter, width)
    gate_mine = swap(in_pieces[0], REP).reshape(width, quarter)
    up_mine = swap(in_pieces[1], REP).reshape(width, quarter)

    upstream = my_cotangent.astype(full) * valid_rows[:, None]

    def to_experts(block):
        sent = block.reshape((1, experts) + block.shape[1:])
        sent = jnp.broadcast_to(sent, (QUAD,) + sent.shape[1:])
        return swap(sent.reshape((QUAD * experts,) + block.shape[1:]), PLANE)

    def dispatch(values):
        return dot(place_any, values).astype(low).reshape(experts, capacity, width)

    expert_upstream = to_experts(dispatch(upstream.astype(low))).reshape(-1, width)
    active_grad_bare = lax.dot_general(
        expert_upstream, down_mine, (((1,), (1,)), ((), ())), preferred_element_type=full
    )

    x_group = group_tokens.astype(full)
    scale_group = lax.rsqrt(jnp.mean(x_group * x_group, axis=-1, keepdims=True) + eps_norm)
    normed_group = (x_group * scale_group * gain_one).astype(low).reshape(exps * rows, width)
    qkv = dot(normed_group, qkv_mine).astype(low).reshape(exps, rows, 3, heads, head_dim)
    queries = qkv[:, :, 0]
    key_rows = qkv[:, :, 1]
    values = qkv[:, :, 2]
    onehot = bucket_onehot(rows)
    bias_mine = lax.dynamic_slice_in_dim(rel_bias, place * heads, heads, 1)
    bias_table = jnp.einsum("ijb,bh->hij", onehot, bias_mine, precision=highest)

    def scores_of():
        raw = (
            jnp.einsum("sihd,sjhd->shij", queries, key_rows, preferred_element_type=full)
            * score_scale
            + bias_table[None]
        )
        return jnp.where(key_ok[:, None, None, :], raw, -1e30)

    scores = scores_of()
    row_max = jnp.max(scores, axis=-1, keepdims=True)
    log_total = row_max + jnp.log(jnp.sum(jnp.exp(scores - row_max), axis=-1, keepdims=True))
    weights_low = jnp.exp(scores - log_total).astype(low)
    context_mine = (
        jnp.einsum("shij,sjhd->sihd", weights_low, values, preferred_element_type=full)
        .astype(low)
        .reshape(exps, rows, head_cols)
    )
    context = jnp.transpose(swap(context_mine, "exp"), (1, 0, 2)).reshape(rows, width)

    x_float = tokens.astype(full)
    scale_one = lax.rsqrt(jnp.mean(x_float * x_float, axis=-1, keepdims=True) + eps_norm)
    hidden_one = x_float + dot(context, full_out)
    scale_two = lax.rsqrt(jnp.mean(hidden_one * hidden_one, axis=-1, keepdims=True) + eps_norm)
    normed_two = (hidden_one * scale_two * gain_two).astype(low)
    normed_float = normed_two.astype(full)
    router_probs = jax.nn.softmax(jnp.dot(normed_float, router, precision=highest), axis=-1)
    picked = jnp.sum(router_probs[:, None, :] * chosen, axis=-1)
    gate_total = jnp.sum(picked, axis=-1, keepdims=True)
    gate_value = picked / gate_total
    combine = gate_value * valid_rows[:, None]
    combine_slots = jnp.sum(
        jnp.where(place_first, combine[None, :, 0], 0.0)
        + jnp.where(place_second, combine[None, :, 1], 0.0),
        axis=1,
    ).reshape(experts, 1, capacity)

    expert_rows = to_experts(dispatch(normed_two)).reshape(-1, width)
    expert_combine = to_experts(combine_slots).reshape(-1, 1)

    gate_part = dot(expert_rows, gate_mine)
    up_part = dot(expert_rows, up_mine)
    active_float, active_pull = jax.vjp(gated_unit, gate_part, up_part)
    active = active_float.astype(low)
    active_scaled = (active_float * expert_combine).astype(low)
    combine_grad_part = jnp.sum(active_float * active_grad_bare, axis=-1).reshape(
        QUAD * experts, 1, capacity
    )
    gate_part_grad, up_part_grad = active_pull(active_grad_bare * expert_combine)
    gate_part_grad = gate_part_grad.astype(low)
    up_part_grad = up_part_grad.astype(low)
    rows_grad_part = (
        lax.dot_general(gate_part_grad, gate_mine, (((1,), (1,)), ((), ())), preferred_element_type=full)
        + lax.dot_general(up_part_grad, up_mine, (((1,), (1,)), ((), ())), preferred_element_type=full)
    ).astype(low)
    output_part = dot(active, down_mine).astype(low)

    combine_grad_back = swap(combine_grad_part, PLANE)
    rows_grad_back = swap(rows_grad_part.reshape(QUAD * experts, capacity, width), PLANE)
    output_back = swap(output_part.reshape(QUAD * experts, capacity, width), PLANE)

    def transposed_dot(a, b):
        return lax.dot_general(a, b, (((0,), (0,)), ((), ())), preferred_element_type=full)

    down_grad = transposed_dot(active_scaled, expert_upstream).astype(low)
    gate_grad = transposed_dot(expert_rows, gate_part_grad).astype(low)
    up_grad = transposed_dot(expert_rows, up_part_grad).astype(low)
    down_share = jnp.sum(
        swap(down_grad.reshape(grps, units, width), "grp").astype(full), axis=0
    )[None]

    def in_columns(grad):
        back = swap(grad.reshape(reps, slab, quarter), REP).astype(full)
        back = jnp.sum(back.reshape(grps, QUAD, slab, grps, units), axis=0)
        return jnp.transpose(back, (1, 2, 0, 3)).reshape(slab, grps * QUAD * units)

    in_share = jnp.concatenate([in_columns(gate_grad), in_columns(up_grad)], axis=1)[None]

    def from_slots(placed, parts):
        hot = jnp.broadcast_to(placed.astype(low)[None], (QUAD,) + placed.shape).reshape(-1, rows)
        return lax.dot_general(
            hot, parts.reshape(-1, width), (((0,), (0,)), ((), ())), preferred_element_type=full
        )

    mixture = combine[:, :1] * from_slots(place_first, output_back) + combine[:, 1:] * from_slots(
        place_second, output_back
    )
    block_loader = (valid_rows[:, None] * (hidden_one + mixture)).astype(low)
    seq_ids = jnp.arange(deal.shape[0], dtype=jnp.int32)
    dealt_seq = jnp.sum(jnp.where(deal == me, seq_ids, 0))
    block_out = lax.dynamic_index_in_dim(
        spread(block_loader, "exp"), dealt_seq - base, 0, keepdims=False
    )

    combine_grad_slots = jnp.sum(combine_grad_back.reshape(QUAD, slots), axis=0)
    combine_grad = jnp.stack(
        [
            jnp.sum(jnp.where(place_first, combine_grad_slots[:, None], 0.0), axis=0),
            jnp.sum(jnp.where(place_second, combine_grad_slots[:, None], 0.0), axis=0),
        ],
        axis=1,
    )
    gate_grad_value = combine_grad * valid_rows[:, None]
    picked_grad = (
        gate_grad_value - jnp.sum(gate_grad_value * gate_value, axis=-1, keepdims=True)
    ) / gate_total
    probs_grad = jnp.sum(picked_grad[:, :, None] * chosen, axis=1)
    logit_grad = router_probs * (
        probs_grad - jnp.sum(probs_grad * router_probs, axis=-1, keepdims=True)
    )
    router_grad = jnp.dot(normed_float.T, logit_grad, precision=highest)
    normed_grad = jnp.dot(logit_grad, router.T, precision=highest) + from_slots(
        jnp.logical_or(place_first, place_second), rows_grad_back
    )
    scaled_two = normed_grad * gain_two
    hidden_grad = (
        upstream
        + scale_two * scaled_two
        - hidden_one * scale_two**3 * jnp.mean(scaled_two * hidden_one, axis=-1, keepdims=True)
    )
    gain_two_grad = jnp.sum(normed_grad * hidden_one * scale_two, axis=0)
    branch_grad = hidden_grad.astype(low)
    context_grad = lax.dot_general(
        branch_grad, full_out, (((1,), (1,)), ((), ())), preferred_element_type=full
    ).astype(low)
    context_grad_pieces = jnp.transpose(context_grad.reshape(rows, exps, head_cols), (1, 0, 2))
    context_grad_mine = swap(context_grad_pieces, "exp").reshape(exps, rows, heads, head_dim)
    branch_group = spread(branch_grad, "exp").reshape(exps * rows, width)
    out_grad = transposed_dot(context_mine.reshape(exps * rows, head_cols), branch_group).astype(low)

    scores = scores_of()
    probs_again = jnp.exp(scores - log_total)
    weights_again = probs_again.astype(low)
    values_grad = jnp.einsum(
        "shij,sihd->sjhd", weights_again, context_grad_mine, preferred_element_type=full
    )
    probs_grad_att = jnp.einsum(
        "sihd,sjhd->shij", context_grad_mine, values, preferred_element_type=full
    )
    row_delta = jnp.sum(probs_grad_att * probs_again, axis=-1, keepdims=True)
    scores_grad = (probs_again * (probs_grad_att - row_delta)).astype(low)
    scores_grad_sum = jnp.sum(scores_grad.astype(full), axis=0)
    bias_grad_mine = jnp.einsum("hij,ijb->bh", scores_grad_sum, onehot, precision=highest)
    bias_grad = lax.dynamic_update_slice_in_dim(
        jnp.zeros((BUCKETS, HEADS), full), bias_grad_mine, place * heads, 1
    )
    queries_grad = (
        jnp.einsum("shij,sjhd->sihd", scores_grad, key_rows, preferred_element_type=full)
        * score_scale
    )
    keys_grad = (
        jnp.einsum("shij,sihd->sjhd", scores_grad, queries, preferred_element_type=full)
        * score_scale
    )
    qkv_grad = (
        jnp.stack([queries_grad, keys_grad, values_grad], axis=2)
        .astype(low)
        .reshape(exps * rows, 3 * head_cols)
    )
    normed_one_part = lax.dot_general(
        qkv_grad, qkv_mine, (((1,), (1,)), ((), ())), preferred_element_type=full
    ).astype(low)
    normed_one_grad = jnp.sum(
        swap(normed_one_part.reshape(exps, rows, width), "exp").astype(full), axis=0
    )
    scaled_one = normed_one_grad * gain_one
    token_grad = (
        hidden_grad
        + scale_one * scaled_one
        - x_float * scale_one**3 * jnp.mean(scaled_one * x_float, axis=-1, keepdims=True)
    )
    gain_one_grad = jnp.sum(normed_one_grad * x_float * scale_one, axis=0)

    qkv_weight_grad = transposed_dot(normed_group, qkv_grad).astype(low)
    qkv_grad_rows = swap(qkv_weight_grad.reshape(exps, row_block, 3 * head_cols), "exp")
    qkv_grad_rows = jnp.transpose(
        qkv_grad_rows.reshape(exps, row_block, 3, head_cols), (1, 2, 0, 3)
    ).reshape(row_block, reps, -1)
    qkv_share = jnp.sum(
        swap(jnp.transpose(qkv_grad_rows, (1, 0, 2)), REP).astype(full), axis=0
    )
    out_pieces = jnp.transpose(out_grad.reshape(row_block, reps, -1), (1, 0, 2))
    out_share = jnp.sum(swap(out_pieces, REP).astype(full), axis=0)

    small = jnp.concatenate(
        [
            router_grad.reshape(-1),
            jnp.stack([gain_one_grad, gain_two_grad], axis=1).reshape(-1),
            bias_grad.reshape(-1),
        ]
    ).reshape(-1, 128)
    small_total = jnp.sum(lax.all_gather(small, ALL, axis=0, tiled=False), axis=0).reshape(-1)
    router_total = small_total[: router.size].reshape(router.shape)
    gains_total = small_total[router.size : router.size + norm_gains.size].reshape(norm_gains.shape)
    bias_total = small_total[router.size + norm_gains.size :].reshape(rel_bias.shape)

    qkv_new = adamw_update(attn_qkv, qkv_first, qkv_second, qkv_share, 1.5 / math.sqrt(D), 0.1)
    out_new = adamw_update(attn_out, out_first, out_second, out_share, 6.0 / math.sqrt(D), 0.1)
    bias_new = adamw_update(rel_bias, bias_first, bias_second, bias_total, 0.3, 0.0)
    router_new = adamw_update(
        router, router_first, router_second, router_total, 1.0 / math.sqrt(D), 0.1
    )
    gains_new = adamw_update(norm_gains, gains_first, gains_second, gains_total, 0.5, 0.0)
    in_new = adamw_update(expert_in, in_first, in_second, in_share, 1.5 / math.sqrt(D), 0.1)
    down_new = adamw_update(
        expert_out, down_first, down_second, down_share, 1.5 / math.sqrt(FF), 0.1
    )
    return (
        (block_out, token_grad)
        + qkv_new
        + out_new
        + bias_new
        + router_new
        + gains_new
        + in_new
        + down_new
    )


def solution(mesh):
    reps, exps = mesh.devices.shape
    split = Mesh(mesh.devices.reshape(reps // QUAD, QUAD, exps), ALL)
    by_rows = P(ALL, None)
    attn = P("exp", REP)
    expert = P("exp", REP, None)
    return jax.shard_map(
        per_device if (reps, exps) == (2 * QUAD, 4) else plain_device,
        mesh=split,
        in_specs=(by_rows, by_rows) + (P(),) * 3 + (attn,) * 6 + (P(),) * 9 + (expert,) * 6,
        out_specs=(by_rows, by_rows) + (attn,) * 6 + (P(),) * 9 + (expert,) * 6,
        check_vma=False,
    )
```

```python
import functools
import math

import jax
import jax.numpy as jnp
from jax import lax
from jax.experimental import pallas as pl
from jax.experimental.pallas import tpu as pltpu
from jax.sharding import Mesh
from jax.sharding import PartitionSpec as P

D = 1024
HEADS = 16
FF = 2816
BUCKETS = 32
STEP = 10
QUAD = 4
REP = ("grp", "quad")
PLANE = ("quad", "exp")
ALL = ("grp", "quad", "exp")

highest = lax.Precision.HIGHEST
eps_norm = 1e-06
thresholds = (1, 2, 3, 4, 5, 6, 7, 8, 11, 16, 22, 32, 45, 64, 90)
beta_one = 0.9
beta_two = 0.999
eps_adam = 1e-08
low = jnp.bfloat16
full = jnp.float32
MESH = pl.DeviceIdType.MESH


def adamw_update(weight, moment, second, gradient, step_rate, decay_factor):
    new_moment = beta_one * moment + (1.0 - beta_one) * gradient
    new_second = beta_two * second + (1.0 - beta_two) * gradient * gradient
    corrected = new_moment / (1.0 - beta_one**STEP)
    scaled = new_second / (1.0 - beta_two**STEP)
    new_weight = weight - step_rate * (
        corrected / (jnp.sqrt(scaled) + eps_adam) + decay_factor * weight
    )
    return (new_moment, new_second, new_weight)


def gated_unit(gate_input, up_input):
    return jax.nn.gelu(gate_input, approximate=True) * up_input


def dot(a, b):
    return jnp.dot(a, b, preferred_element_type=full)


def nt(a, b, precision=None):
    return lax.dot_general(a, b, (((1,), (1,)), ((), ())), preferred_element_type=full, precision=precision)


def tn(a, b):
    return lax.dot_general(a, b, (((0,), (0,)), ((), ())), preferred_element_type=full)


class Where:
    def __init__(self, grps, exps):
        self.grps, self.exps = grps, exps
        self.reps = grps * QUAD
        self.grp = lax.axis_index("grp")
        self.quad = lax.axis_index("quad")
        self.exp = lax.axis_index("exp")
        self.rep = self.grp * QUAD + self.quad
        self.base = self.rep * exps
        self.me = self.base + self.exp

    def device(self, rep, exp):
        return (rep // QUAD, rep % QUAD, exp)

    def near(self, flip):
        q = self.quad
        if flip & 1:
            q = q + 1 - 2 * (q % 2)
        if flip & 2:
            q = q + 2 - 4 * (q // 2)
        return q


def send(src, dst, send_sem, recv_sem, device):
    return pltpu.make_async_remote_copy(
        src_ref=src, dst_ref=dst, send_sem=send_sem, recv_sem=recv_sem, device_id=device, device_id_type=MESH
    )


def arrived(ref, sem):
    pltpu.make_async_copy(ref, ref, sem).wait()


def greet_all(at):
    count = at.reps * at.exps
    barrier = pltpu.get_barrier_semaphore()

    def greet(k, _):
        other = (at.me + k) % count
        pl.semaphore_signal(
            barrier, inc=1, device_id=at.device(other // at.exps, other % at.exps), device_id_type=MESH
        )
        return 0

    lax.fori_loop(1, count, greet, 0)
    pl.semaphore_wait(barrier, count - 1)


def turn(exp, i):
    beside = exp + 1 - 2 * (exp % 2)
    return jnp.where(i == 0, (beside + 2) % 4, jnp.where(i == 1, (exp + 2) % 4, jnp.where(i == 2, beside, exp)))


def lane_of(shape):
    return lax.broadcasted_iota(jnp.int32, shape, 1)


def row_of(shape):
    return lax.broadcasted_iota(jnp.int32, shape, 0)


def bucket_of(offset):
    distance = jnp.abs(offset)
    bucket = jnp.where(offset > 0, 16, 0)
    for threshold in thresholds:
        bucket = bucket + jnp.where(distance >= threshold, 1, 0)
    return bucket


def bits_of(count):
    return count.bit_length() - 1


def column_parts(width):
    tiles = width // 128
    cuts = [0, (tiles + 2) // 3, (2 * tiles + 2) // 3, tiles]
    return [(cuts[i] * 128, (cuts[i + 1] - cuts[i]) * 128) for i in range(3)]


def flipped(place, bit):
    return place + (1 - 2 * ((place // (1 << bit)) % 2)) * (1 << bit)


class Doubling:
    def __init__(self, at, own, every, sems, core_sems, orders):
        self.at, self.own, self.every = at, own, every
        self.sems, self.core_sems, self.orders = sems, core_sems, orders
        self.plane = at.quad * at.exps + at.exp
        self.steps = len(orders[0])
        self.parts = column_parts(own.shape[1])

    def device(self, bit):
        other = flipped(self.plane, bit)
        return (self.at.grp, other // self.at.exps, other % self.at.exps)

    def place(self, part, j):
        p = self.plane
        for i, bit in enumerate(self.orders[part]):
            if (j >> i) & 1:
                p = flipped(p, bit + 1)
        return p

    def block(self, part, p):
        begin, size = self.parts[part]
        return self.every.at[p, :, pl.ds(begin, size)]

    def source(self, part, j):
        begin, size = self.parts[part]
        return self.own.at[:, pl.ds(begin, size)] if j == 0 else self.block(part, self.place(part, j))

    def index(self, step, part, j):
        return part * (1 << self.steps) + (1 << step) - 1 + j

    def copy(self, step, part, j):
        i = self.index(step, part, j)
        return send(
            self.source(part, j),
            self.block(part, self.place(part, j)),
            self.sems.at[0, i],
            self.sems.at[1, i],
            self.device(self.orders[part][step] + 1),
        )

    def core_copy(self, part, j):
        i = part * (1 << self.steps) + j
        return send(
            self.source(part, j),
            self.block(part, self.place(part, j)),
            self.core_sems.at[0, i],
            self.core_sems.at[1, i],
            self.device(0),
        )

    def start(self):
        for part in range(3):
            for step in range(self.steps):
                self.copy(step, part, 0).start()
        for part in range(3):
            self.core_copy(part, 0).start()
        self.keep().start()

    def keep(self):
        return pltpu.make_async_copy(self.own, self.every.at[self.plane], self.core_sems.at[1, 3 << self.steps])

    def next(self, step):
        for part in range(3):
            for j in range(1 << step):
                k = (1 << step) + j
                arrived(self.block(part, self.place(part, k)), self.sems.at[1, self.index(step, part, j)])
                for later in range(step + 1, self.steps):
                    self.copy(later, part, k).start()
                self.core_copy(part, k).start()

    def finish_in(self):
        for part in range(3):
            for j in range(1 << self.steps):
                there = self.block(part, flipped(self.place(part, j), 0))
                arrived(there, self.core_sems.at[1, part * (1 << self.steps) + j])
        self.keep().wait()

    def finish_out(self):
        for part in range(3):
            for j in range(1 << self.steps):
                self.core_copy(part, j).wait_send()
            for step in range(self.steps):
                for j in range(1 << step):
                    self.copy(step, part, j).wait_send()


class Group:
    def __init__(self, at, own, every, sems):
        self.at, self.own, self.every, self.sems = at, own, every, sems
        self.beside, self.across = at.exp + 1 - 2 * (at.exp % 2), (at.exp + 2) % 4

    def copy(self, src, index, send_index, device):
        return send(
            src, self.every.at[index], self.sems.at[0, send_index], self.sems.at[1, index], self.at.device(self.at.rep, device)
        )

    def first(self):
        return [
            self.copy(self.own, self.at.exp, 0, self.across),
            self.copy(self.own, self.at.exp, 1, self.beside),
        ]

    def second(self):
        return self.copy(self.every.at[self.across], self.across, 2, self.beside)

    def start(self):
        for copy in self.first():
            copy.start()

    def pass_on(self):
        arrived(self.every.at[self.across], self.sems.at[1, self.across])
        self.second().start()

    def arrive(self):
        for index in (self.beside, (self.beside + 2) % 4):
            arrived(self.every.at[index], self.sems.at[1, index])

    def sent(self):
        for copy in self.first() + [self.second()]:
            copy.wait_send()


class Tiles:
    def __init__(self, units, reps):
        self.units = units
        self.reps = reps
        self.hidden = units * reps
        self.half = self.hidden // 256
        self.wide = (self.half + 1) // 2
        self.count = 3
        self.size = 128 * self.wide // self.count
        self.skip = 128 * (2 * self.wide - self.half)

    def start(self, quad):
        return 128 * (self.half * (quad // 2) + (self.half - self.wide) * (quad % 2))

    def rows(self, tile):
        result = []
        for k in range(QUAD):
            found = None
            for parity in range(2):
                first = self.start(parity) + tile * self.size
                live = first + (self.skip if parity and tile == 0 else 0)
                begin = max(live, k * self.units)
                end = min(first + self.size, (k + 1) * self.units)
                if end > begin:
                    found = (begin - k * self.units, end - begin, parity, begin - first)
            result.append(found)
        return result


class Outward:
    def __init__(self, at, tiles, tile, in_low, down_slab, both_w, down_w, nothing, sems, down_sems):
        self.at, self.tiles, self.tile = at, tiles, tile
        self.in_low, self.down_slab, self.both_w, self.down_w = in_low, down_slab, both_w, down_w
        self.nothing, self.sems, self.down_sems = nothing, sems, down_sems
        self.slab = in_low.shape[0]

    def source(self, quad, section):
        begin = section * self.tiles.hidden + self.tiles.start(quad) + self.tile * self.tiles.size
        return self.in_low.at[:, pl.ds(pl.multiple_of(begin, 128), self.tiles.size)]

    def target(self, rep, section):
        rows = pl.ds(pl.multiple_of(rep * self.slab, self.slab), self.slab)
        return self.both_w.at[rows, pl.ds(section * self.tiles.size, self.tiles.size)]

    def over(self, act):
        at = self.at

        def one(k, _):
            other = (at.rep + k) % at.reps
            for section in range(2):
                act(
                    functools.partial(
                        send,
                        self.source(other % QUAD, section),
                        self.target(at.rep, section),
                        self.sems.at[0, section * at.reps + other],
                        self.sems.at[1, section * at.reps + at.rep],
                        at.device(other, at.exp),
                    )
                )
            return 0

        lax.fori_loop(1, at.reps, one, 0)

    def over_down(self, act, act_local):
        at = self.at
        for k, piece in enumerate(self.tiles.rows(self.tile)):
            if piece is None:
                continue
            begin, count, parity, to = piece
            quad = 2 * (at.rep // QUAD) + parity
            src, dst = self.down_slab.at[pl.ds(begin, count)], self.down_w.at[pl.ds(to, count)]
            recv = self.down_sems.at[1, at.rep]
            for g in range(at.grps):
                stays = jnp.logical_and(at.grp == g, at.quad == quad)
                ours = at.rep % QUAD == k

                @pl.when(jnp.logical_and(ours, jnp.logical_not(stays)))
                def _():
                    act(functools.partial(send, src, dst, self.down_sems.at[0, g], recv, (g, quad, at.exp)))

                @pl.when(jnp.logical_and(ours, stays))
                def _():
                    act_local(functools.partial(pltpu.make_async_copy, src, dst, recv))

    def blank(self):
        return pltpu.make_async_copy(
            self.nothing, self.down_w.at[pl.ds(0, self.tiles.skip)], self.down_sems.at[1, self.at.reps]
        )

    def start(self):
        at = self.at
        self.over_down(lambda copy: copy().start(), lambda copy: copy().start())
        self.over(lambda copy: copy().start())
        for section in range(2):
            pltpu.make_async_copy(
                self.source(at.quad, section), self.target(at.rep, section), self.sems.at[1, section * at.reps + at.rep]
            ).start()
        if self.tile == 0:

            @pl.when(at.quad % 2 == 1)
            def _():
                self.blank().start()

    def arrive(self):
        at = self.at

        def one(rep, _):
            for section in range(2):
                arrived(self.target(rep, section), self.sems.at[1, section * at.reps + rep])
            return 0

        lax.fori_loop(0, at.reps, one, 0)
        for parity in range(2):

            @pl.when(at.quad % 2 == parity)
            def _():
                for k, piece in enumerate(self.tiles.rows(self.tile)):
                    if piece is not None and piece[2] == parity:
                        source = QUAD * (at.quad // 2) + k
                        arrived(self.down_w.at[pl.ds(piece[3], piece[1])], self.down_sems.at[1, source])
                if parity and self.tile == 0:
                    self.blank().wait()

    def sent(self):
        self.over(lambda copy: copy().wait_send())
        self.over_down(lambda copy: copy().wait_send(), lambda copy: None)


class Homeward:
    def __init__(self, at, tiles, tile, both, down, in_parts, down_parts, sems, down_sems):
        self.at, self.tiles, self.tile = at, tiles, tile
        self.both, self.down, self.in_parts, self.down_parts = both, down, in_parts, down_parts
        self.sems, self.down_sems = sems, down_sems
        self.slab = in_parts.shape[1]

    def target(self, grp, quad, parity, section):
        skip = self.tiles.skip if parity and self.tile == 0 else 0
        to = section * self.tiles.hidden + self.tiles.start(quad) + self.tile * self.tiles.size + skip
        to = to if isinstance(to, int) else pl.multiple_of(to, 128)
        return skip, self.in_parts.at[grp, :, pl.ds(to, self.tiles.size - skip)]

    def copy(self, rep, parity, section, local=False):
        at = self.at
        skip, dst = self.target(at.grp, at.quad, parity, section)
        rows = pl.ds(pl.multiple_of(rep * self.slab, self.slab), self.slab)
        src = self.both.at[rows, pl.ds(section * self.tiles.size + skip, self.tiles.size - skip)]
        recv = self.sems.at[1, section * at.reps + at.rep]
        if local:
            return pltpu.make_async_copy(src, dst, recv)
        return send(src, dst, self.sems.at[0, section * at.reps + rep], recv, at.device(rep, at.exp))

    def over(self, act, act_local):
        at = self.at
        for parity in range(2):

            @pl.when(at.quad % 2 == parity)
            def _():
                def one(k, _):
                    for section in range(2):
                        act(self.copy((at.rep + k) % at.reps, parity, section))
                    return 0

                lax.fori_loop(1, at.reps, one, 0)
                if act_local:
                    for section in range(2):
                        act_local(self.copy(at.rep, parity, section, local=True))

    def over_down(self, act, act_local):
        at = self.at
        for k, piece in enumerate(self.tiles.rows(self.tile)):
            if piece is None:
                continue
            begin, count, parity, to = piece
            src, dst = self.down.at[pl.ds(to, count)], self.down_parts.at[at.grp, pl.ds(begin, count)]
            recv = self.down_sems.at[1, at.grp]
            stays = jnp.logical_and(at.grp == at.quad // 2, at.quad == k)
            ours = at.quad % 2 == parity

            @pl.when(jnp.logical_and(ours, jnp.logical_not(stays)))
            def _():
                act(functools.partial(send, src, dst, self.down_sems.at[0, k], recv, (at.quad // 2, k, at.exp)))

            @pl.when(jnp.logical_and(ours, stays))
            def _():
                act_local(functools.partial(pltpu.make_async_copy, src, dst, recv))

    def start(self):
        self.over_down(lambda copy: copy().start(), lambda copy: copy().start())
        self.over(lambda copy: copy.start(), lambda copy: copy.start())

    def arrive(self):
        at = self.at
        for rep in range(at.reps):
            for section in range(2):
                _, dst = self.target(rep // QUAD, rep % QUAD, rep % 2, section)
                arrived(dst, self.sems.at[1, section * at.reps + rep])
        for k, piece in enumerate(self.tiles.rows(self.tile)):
            if piece is None:
                continue

            @pl.when(at.quad == k)
            def _():
                for g in range(at.grps):
                    arrived(self.down_parts.at[g, pl.ds(piece[0], piece[1])], self.down_sems.at[1, g])

    def sent(self):
        self.over(lambda copy: copy.wait_send(), None)
        self.over_down(lambda copy: copy().wait_send(), lambda copy: None)


def forward_kernel(
    grps,
    exps,
    lengths,
    bias_table,
    routes_t,
    tokens,
    cotangent,
    gains,
    router,
    qkv_t,
    out_w,
    in_low,
    down_slab,
    both_w,
    down_w,
    cot_all,
    n_all,
    comb_all,
    qkv_out,
    lse_out,
    mine_out,
    n1_out,
    wqkv_out,
    wout_out,
    h1_out,
    n2_out,
    probs_out,
    tok_all,
    wqkv,
    wout,
    n1,
    qkv,
    lse,
    mine,
    ctx,
    bias,
    comb_send,
    nothing,
    tok_sem,
    wq_sem,
    wo_sem,
    wo2_sem,
    weight_sem,
    down_sem,
    ctx_sem,
    cot_sem,
    cot_core_sem,
    n_sem,
    n_core_sem,
    comb_sem,
    store_sem,
):
    at = Where(grps, exps)
    reps = at.reps
    rows, width = tokens.shape
    heads = HEADS // exps
    head_dim = width // HEADS
    head_cols = heads * head_dim
    block_cols = min(128, head_cols)
    shard_cols, row_block = qkv_t.shape
    seg = math.gcd(shard_cols, head_cols)
    segs = shard_cols // seg
    tiles = Tiles(down_slab.shape[0], reps)
    plane = at.quad * exps + at.exp
    members = QUAD * exps
    scale = 1.0 / math.sqrt(head_dim)
    SEND, RECV = 0, 1

    greet_all(at)

    def exp_peer(k):
        return (at.exp + k) % exps

    group_tokens = Group(at, tokens, tok_all, tok_sem)
    group_tokens.start()
    tok_all[at.exp] = tokens[...]

    def segment(k):
        col = (at.rep * segs + k) * seg
        section = col // width
        within = col - section * width
        owner = within // head_cols
        return owner, section * head_cols + within - owner * head_cols

    def segment_copy(k, shift):
        owner, offset = segment(k)
        src = qkv_t.at[pl.ds(k * seg, seg)]
        dst = wqkv.at[at.exp, pl.ds(pl.multiple_of(offset, seg), seg)]
        target = at.device((at.rep + shift) % reps, owner)
        return owner, src, dst, functools.partial(
            send, src, dst, wq_sem.at[SEND, k * reps + shift], wq_sem.at[RECV, at.exp * 3 * (head_cols // seg) + offset // seg], target
        )

    def over_segments(act, act_local):
        def one(i, _):
            k, shift = i // reps, i % reps
            owner, src, dst, copy = segment_copy(k, shift)
            stays = jnp.logical_and(shift == 0, owner == at.exp)

            @pl.when(jnp.logical_not(stays))
            def _():
                act(copy())

            @pl.when(stays)
            def _():
                act_local(k, src, dst)

            return 0

        lax.fori_loop(0, segs * reps, one, 0)

    def local_segment(k, src, dst):
        _, offset = segment(k)
        pltpu.make_async_copy(src, dst, wq_sem.at[RECV, at.exp * 3 * (head_cols // seg) + offset // seg]).start()

    over_segments(lambda copy: copy.start(), local_segment)

    for k in range(1, reps):
        other = (at.rep + k) % reps
        send(
            out_w, wout.at[at.exp, at.rep], wo_sem.at[SEND, other], wo_sem.at[RECV, at.rep], at.device(other, at.exp)
        ).start()
    wout[at.exp, at.rep] = out_w[...]
    chip_bits = list(range(bits_of(members) - 1))
    cots = Doubling(at, cotangent, cot_all, cot_sem, cot_core_sem, [chip_bits[::-1]] * 3)
    cots.start()

    span = 2 * rows
    bucket = bucket_of(lane_of((8, span)) - rows)
    for h in range(heads):
        line = jnp.zeros((8, span), full)
        for b in range(BUCKETS):
            line = jnp.where(bucket == b, bias_table[at.exp * heads + h, b], line)
        whole = jnp.broadcast_to(line[0:1], (rows, span))
        bias[h] = pltpu.roll(whole, 0, 1, stride=1, stride_axis=0)[:, rows:]

    group_tokens.pass_on()
    group_tokens.arrive()

    def norm_group(s, _):
        x = tok_all[s].astype(full)
        r = lax.rsqrt(jnp.mean(x * x, axis=1, keepdims=True) + eps_norm)
        n1[s] = (x * r * gains[0:1, :]).astype(low)
        return 0

    lax.fori_loop(0, exps, norm_group, 0)

    nothing[...] = jnp.zeros_like(nothing)
    weights = [
        Outward(
            at, tiles, t, in_low, down_slab, both_w.at[t], down_w.at[t], nothing, weight_sem.at[t], down_sem.at[t]
        )
        for t in range(2)
    ]
    weights[0].start()

    def wait_segment(i, _):
        e, j = i // (3 * head_cols // seg), i % (3 * head_cols // seg)
        arrived(wqkv.at[e, pl.ds(pl.multiple_of(j * seg, seg), seg)], wq_sem.at[RECV, i])
        return 0

    lax.fori_loop(0, exps * 3 * head_cols // seg, wait_segment, 0)

    def project(s, _):
        total = jnp.zeros((rows, 3 * head_cols), full)
        for e in range(exps):
            total = total + nt(n1[s, :, e * row_block : (e + 1) * row_block], wqkv[e])
        qkv[s] = total.astype(low)
        return 0

    lax.fori_loop(0, exps, project, 0)

    group_wout = Group(at, wout.at[at.exp], wout, wo2_sem)

    def beside(k):
        if k == 1:
            for j in range(1, reps):
                other = (at.rep + j) % reps
                arrived(wout.at[at.exp, other], wo_sem.at[RECV, other])
            group_wout.start()
        elif k == 2:
            cots.next(0)
        else:
            group_wout.pass_on()

    def attend(i, _):
        s = turn(at.exp, i)
        for k in range(1, exps):

            @pl.when(i == k)
            def _():
                beside(k)

        ok = lane_of((rows, rows)) < lengths[at.base + s]
        lane = lane_of((rows, block_cols))
        sums = jnp.zeros((rows, 128), full)
        for c in range(head_cols // block_cols):
            cols = slice(c * block_cols, (c + 1) * block_cols)
            q = qkv[s, :, cols] * scale
            k = qkv[s, :, head_cols + c * block_cols : head_cols + (c + 1) * block_cols]
            v = qkv[s, :, 2 * head_cols + c * block_cols : 2 * head_cols + (c + 1) * block_cols]
            result = jnp.zeros((rows, block_cols), full)
            for t in range(block_cols // head_dim):
                h = c * (block_cols // head_dim) + t
                here = jnp.logical_and(lane >= t * head_dim, lane < (t + 1) * head_dim)
                scores = nt(jnp.where(here, q, jnp.zeros_like(q)), k) + bias[h]
                scores = jnp.where(ok, scores, -1e30)
                top = jnp.max(scores, axis=1, keepdims=True)
                weights = jnp.exp(scores - top)
                total = jnp.sum(weights, axis=1, keepdims=True)
                weights = (weights * (1.0 / total)).astype(low)
                result = jnp.where(here, jnp.dot(weights, v, preferred_element_type=full), result)
                sums = jnp.where(lane_of((rows, 128)) == h, top + jnp.log(total), sums)
            mine[s, :, cols] = result.astype(low)
        lse[s] = sums

        @pl.when(i < exps - 1)
        def _():
            send(
                mine.at[s], ctx.at[at.exp], ctx_sem.at[SEND, s], ctx_sem.at[RECV, at.exp], at.device(at.rep, s)
            ).start()

        @pl.when(i == exps - 1)
        def _():
            pltpu.make_async_copy(mine.at[s], ctx.at[at.exp], ctx_sem.at[RECV, at.exp]).start()

        return 0

    lax.fori_loop(0, exps, attend, 0)

    cots.next(1)
    group_wout.arrive()
    for e in range(exps):
        arrived(ctx.at[e], ctx_sem.at[RECV, e])

    out_cols = wout.shape[3]
    for r in range(reps):
        cols = slice(r * out_cols, (r + 1) * out_cols)
        total = tokens[:, cols].astype(full)
        for e in range(exps):
            total = total + jnp.dot(ctx[e], wout[e, r], preferred_element_type=full)
        h1_out[:, cols] = total
    h1 = h1_out[...]
    r2 = lax.rsqrt(jnp.mean(h1 * h1, axis=1, keepdims=True) + eps_norm)
    n2 = (h1 * r2 * gains[1:2, :]).astype(low)
    n2_out[...] = n2
    rotated = [chip_bits[c:] + chip_bits[:c] for c in range(3)]
    rows_two = Doubling(at, n2_out, n_all, n_sem, n_core_sem, rotated)
    rows_two.start()
    weights[1].start()

    router_rows = jnp.concatenate([router[...], jnp.zeros((128 - exps, width), full)], axis=0)
    logits = nt(n2.astype(full), router_rows, precision=highest)
    lane = lane_of((rows, 128))
    logits = jnp.where(lane < exps, logits, -1e30)
    probs = jnp.exp(logits - jnp.max(logits, axis=1, keepdims=True))
    probs = probs / jnp.sum(probs, axis=1, keepdims=True)
    probs_out[...] = probs
    picked = jnp.where(routed(routes_t, at.me, rows), probs, 0.0)
    comb = picked / jnp.sum(picked, axis=1, keepdims=True)
    comb = jnp.where(row_of((rows, 1)) < lengths[at.me], comb, 0.0)
    comb_send[...] = comb.T[0 : comb_send.shape[0]]

    def comb_copy(k):
        other = (plane + k) % members
        return send(
            comb_send,
            comb_all.at[plane],
            comb_sem.at[SEND, other],
            comb_sem.at[RECV, plane],
            (at.grp, other // exps, other % exps),
        )

    def start_comb(k, _):
        comb_copy(k).start()
        return 0

    lax.fori_loop(1, members, start_comb, 0)
    pltpu.make_async_copy(comb_send, comb_all.at[plane], comb_sem.at[RECV, plane]).start()
    rows_two.next(0)

    stores = [
        (qkv, qkv_out),
        (lse, lse_out),
        (mine, mine_out),
        (n1, n1_out),
        (wqkv, wqkv_out),
        (wout, wout_out),
    ]
    for i, (src, dst) in enumerate(stores):
        pltpu.make_async_copy(src, dst, store_sem.at[i]).start()

    for step in range(1, rows_two.steps):
        rows_two.next(step)
    for step in range(2, cots.steps):
        cots.next(step)

    cots.finish_in()
    rows_two.finish_in()

    def comb_in(k, _):
        arrived(comb_all.at[k], comb_sem.at[RECV, k])
        return 0

    lax.fori_loop(0, members, comb_in, 0)
    for tile in weights:
        tile.arrive()

    for k in range(1, exps):
        peer = exp_peer(k)
        arrived(mine.at[peer], ctx_sem.at[SEND, peer])
    over_segments(lambda copy: copy.wait_send(), lambda k, src, dst: None)
    for k in range(1, reps):
        arrived(out_w, wo_sem.at[SEND, (at.rep + k) % reps])
    group_tokens.sent()
    group_wout.sent()
    cots.finish_out()
    rows_two.finish_out()

    def sent_comb(k, _):
        comb_copy(k).wait_send()
        return 0

    lax.fori_loop(1, members, sent_comb, 0)
    for tile in weights:
        tile.sent()
    for i, (src, dst) in enumerate(stores):
        pltpu.make_async_copy(src, dst, store_sem.at[i]).wait()


def forward_call(
    grps, exps, lengths, bias_table, routes_t, tokens, cotangent, gains, router, qkv_t, out_w, in_low, down_slab
):
    reps = grps * QUAD
    rows, width = tokens.shape
    head_cols = width // exps
    row_block = qkv_t.shape[1]
    seg = math.gcd(qkv_t.shape[0], head_cols)
    segs = qkv_t.shape[0] // seg
    units = down_slab.shape[0]
    out_cols = out_w.shape[1]
    heads = HEADS // exps
    members = QUAD * exps
    tiles = Tiles(units, reps)
    shape = jax.ShapeDtypeStruct
    vmem = pl.BlockSpec(memory_space=pltpu.VMEM)
    smem = pl.BlockSpec(memory_space=pltpu.SMEM)
    hbm = pl.BlockSpec(memory_space=pl.ANY)
    results = [
        (shape((2, width, 2 * tiles.size), low), hbm),
        (shape((2, tiles.size, width), low), hbm),
        (shape((members, rows, width), low), hbm),
        (shape((members, rows, width), low), hbm),
        (shape((members, 8, rows), full), hbm),
        (shape((exps, rows, 3 * head_cols), low), hbm),
        (shape((exps, rows, 128), full), hbm),
        (shape((exps, rows, head_cols), low), hbm),
        (shape((exps, rows, width), low), hbm),
        (shape((exps, 3 * head_cols, row_block), low), hbm),
        (shape((exps, reps, row_block, out_cols), low), hbm),
        (shape((rows, width), full), vmem),
        (shape((rows, width), low), vmem),
        (shape((rows, 128), full), vmem),
    ]
    dma = pltpu.SemaphoreType.DMA
    chips = members // 2
    return pl.pallas_call(
        functools.partial(forward_kernel, grps, exps),
        out_shape=[r[0] for r in results],
        in_specs=[smem] * 2 + [vmem] * 7 + [hbm] * 2,
        out_specs=[r[1] for r in results],
        scratch_shapes=[
            pltpu.VMEM((exps, rows, width), low),
            pltpu.VMEM((exps, 3 * head_cols, row_block), low),
            pltpu.VMEM((exps, reps, row_block, out_cols), low),
            pltpu.VMEM((exps, rows, width), low),
            pltpu.VMEM((exps, rows, 3 * head_cols), low),
            pltpu.VMEM((exps, rows, 128), full),
            pltpu.VMEM((exps, rows, head_cols), low),
            pltpu.VMEM((exps, rows, head_cols), low),
            pltpu.VMEM((heads, rows, rows), full),
            pltpu.VMEM((8, rows), full),
            pltpu.VMEM((tiles.skip, width), low),
            dma((2, exps)),
            dma((2, max(segs * reps, exps * 3 * head_cols // seg))),
            dma((2, reps)),
            dma((2, exps)),
            dma((2, 2, 2 * reps)),
            dma((2, 2, reps + 1)),
            dma((2, exps)),
            dma((2, 3 * chips)),
            dma((2, 3 * chips + 1)),
            dma((2, 3 * chips)),
            dma((2, 3 * chips + 1)),
            dma((2, members)),
            dma((6,)),
        ],
        compiler_params=pltpu.CompilerParams(
            collective_id=0, has_side_effects=True, vmem_limit_bytes=60 * 1024 * 1024
        ),
        name="forward",
    )(lengths, bias_table, routes_t, tokens, cotangent, gains, router, qkv_t, out_w, in_low, down_slab)


def expert_kernel(
    grps,
    exps,
    cap,
    deal,
    routes_t,
    comb,
    n_all,
    cot_all,
    both_w,
    down_w,
    in_low,
    down_slab,
    n_sum,
    y_sum,
    c_sum,
    both_g,
    down_g,
    in_parts,
    down_parts,
    place,
    marks,
    n_rows,
    g_rows,
    both_v,
    down_v,
    raw_n,
    raw_g,
    y_acc,
    n_acc,
    both_d,
    active,
    both_stage,
    down_stage,
    out_n,
    out_y,
    load_sem,
    raw_sem,
    out_sem,
    in_sem,
    in_down_sem,
    home_sem,
    home_down_sem,
    stage_sem,
):
    at = Where(grps, exps)
    rows, width = n_all.shape[1:]
    tiles = Tiles(down_slab.shape[0], at.reps)
    size = tiles.size
    slots = exps * cap
    members = QUAD * exps
    loads = [pltpu.make_async_copy(both_w.at[t], both_v.at[t], load_sem.at[0, t]) for t in range(2)] + [
        pltpu.make_async_copy(down_w.at[t], down_v.at[t], load_sem.at[1, t]) for t in range(2)
    ]
    for copy in loads:
        copy.start()

    def raw_copies(q):
        here = pl.ds(pl.multiple_of(q * exps, exps), exps)
        return [
            pltpu.make_async_copy(n_all.at[here], raw_n.at[q % 2], raw_sem.at[0, q % 2]),
            pltpu.make_async_copy(cot_all.at[here], raw_g.at[q % 2], raw_sem.at[1, q % 2]),
        ]

    for copy in raw_copies(0):
        copy.start()
    greet_all(at)
    last = tiles.count - 1
    incoming = Outward(
        at, tiles, last, in_low, down_slab, both_v.at[last], down_v.at[last], None, in_sem, in_down_sem
    )
    incoming.start()
    home = Homeward(
        at, tiles, 0, both_stage.at[0], down_stage.at[0], in_parts, down_parts, home_sem, home_down_sem
    )

    earlier = jnp.where(row_of((rows, rows)) < lane_of((rows, rows)), 1.0, 0.0).astype(low)
    slot = row_of((cap, rows)).astype(full)

    def dispatch(q, _):
        @pl.when(q + 1 < QUAD)
        def _():
            for copy in raw_copies(q + 1):
                copy.start()

        for copy in raw_copies(q):
            copy.wait()
        lines = []
        for j in range(exps):
            seq = at.grp * members + q * exps + j
            pair = routes_t[:, pl.ds(pl.multiple_of(seq * rows, rows), rows)]
            lines.append(jnp.logical_or(pair[0:1] == at.exp, pair[1:2] == at.exp))
        lines = [jnp.where(line, 1.0, 0.0) for line in lines] + [jnp.zeros((8 - exps, rows), full)]
        hot_low = jnp.concatenate(lines, axis=0).astype(low)
        before = dot(hot_low, earlier)
        for j in range(exps):
            s = q * exps + j
            inside = jnp.logical_and(slot == before[j : j + 1, :], hot_low[j : j + 1, :].astype(full) > 0.5)
            here = jnp.where(inside, 1.0, 0.0)
            place[s] = here.astype(low)
            g = raw_g[q % 2, 0]
            for b in range(1, exps):
                g = jnp.where(deal[at.grp * members + s] == at.grp * members + q * exps + b, raw_g[q % 2, b], g)
            where = pl.ds(pl.multiple_of(s * cap, cap), cap)
            n_rows[where] = dot(here.astype(low), raw_n[q % 2, j]).astype(low)
            g_rows[where] = dot(here.astype(low), g).astype(low)
            marks[where, 0:1] = jnp.sum(here * comb[s, pl.ds(at.exp, 1), :], axis=1, keepdims=True)
            marks[where, 1:2] = jnp.zeros((cap, 1), full)
        return 0

    lax.fori_loop(0, QUAD, dispatch, 0)
    for copy in loads:
        copy.wait()
    curve = math.sqrt(2.0 / math.pi)

    def tile_work(f, _):
        @pl.when(f == last)
        def _():
            incoming.arrive()

        def chunk(c, _):
            here = pl.ds(pl.multiple_of(c * slots, slots), slots)
            share = marks[here, 0:1]
            both = dot(n_rows[here], both_v[f])
            gate_part, up_part = both[:, :size], both[:, size:]
            grad = nt(g_rows[here], down_v[f])
            square = gate_part * gate_part
            bend = jnp.tanh(curve * gate_part * (1.0 + 0.044715 * square))
            half = 0.5 * (1.0 + bend)
            gelu = gate_part * half
            slope = half + (0.5 * curve) * gate_part * (1.0 - bend * bend) * (1.0 + (3 * 0.044715) * square)
            value = gelu * up_part
            marks[here, 1:2] += jnp.sum(value * grad, axis=1, keepdims=True)
            grad = grad * share
            active[here] = (value * share).astype(low)
            both_d[here, :size] = (grad * up_part * slope).astype(low)
            both_d[here, size:] = (grad * gelu).astype(low)
            y = dot(active[here], down_v[f])
            y_acc[here] = jnp.where(f == 0, y, y_acc[here].astype(full) + y).astype(low)
            n_back = nt(both_d[here], both_v[f])
            n_acc[here] = jnp.where(f == 0, n_back, n_acc[here] + n_back)
            return 0

        lax.fori_loop(0, QUAD, chunk, 0)

        def columns(m, _):
            cols = pl.ds(pl.multiple_of(m * (width // 2), width // 2), width // 2)
            both_stage[f, cols] = tn(n_rows[:, cols], both_d[...]).astype(low)
            down_stage[f, :, cols] = tn(active[...], g_rows[:, cols]).astype(low)
            return 0

        lax.fori_loop(0, 2, columns, 0)

        @pl.when(f == 0)
        def _():
            home.start()

        @pl.when(f > 0)
        def _():
            for copy in stage_copies(f):
                copy.start()

        return 0

    def stage_copies(f):
        return [
            pltpu.make_async_copy(both_stage.at[f], both_g.at[f - 1], stage_sem.at[0, f]),
            pltpu.make_async_copy(down_stage.at[f], down_g.at[f - 1], stage_sem.at[1, f]),
        ]

    lax.fori_loop(0, tiles.count, tile_work, 0)

    def out_copies(s):
        return [
            pltpu.make_async_copy(out_n.at[s % 2], n_sum.at[s], out_sem.at[0, s % 2]),
            pltpu.make_async_copy(out_y.at[s % 2], y_sum.at[s], out_sem.at[1, s % 2]),
        ]

    def gather(s, _):
        @pl.when(s >= 2)
        def _():
            for copy in out_copies(s - 2):
                copy.wait()

        where = pl.ds(pl.multiple_of(s * cap, cap), cap)
        out_n[s % 2] = tn(place[s], n_acc[where].astype(low)).astype(low)
        out_y[s % 2] = tn(place[s], y_acc[where]).astype(low)
        line = jnp.sum(place[s].astype(full) * marks[where, 1:2], axis=0, keepdims=True)
        c_sum[s] = jnp.broadcast_to(line, (8, rows))
        for copy in out_copies(s):
            copy.start()
        return 0

    lax.fori_loop(0, members, gather, 0)
    for s in (members - 2, members - 1):
        for copy in out_copies(s):
            copy.wait()
    for f in range(1, tiles.count):
        for copy in stage_copies(f):
            copy.wait()
    home.arrive()
    incoming.sent()
    home.sent()


def expert_call(grps, exps, cap, deal, routes_t, comb_all, n_all, cot_all, both_w, down_w, in_low, down_slab):
    members, rows, width = n_all.shape
    reps = grps * QUAD
    tiles = Tiles(down_slab.shape[0], reps)
    size = tiles.size
    slab, both_hidden = in_low.shape
    units = down_slab.shape[0]
    slots = exps * cap
    shape = jax.ShapeDtypeStruct
    vmem = pl.BlockSpec(memory_space=pltpu.VMEM)
    smem = pl.BlockSpec(memory_space=pltpu.SMEM)
    hbm = pl.BlockSpec(memory_space=pl.ANY)
    results = [
        (shape((members, rows, width), low), hbm),
        (shape((members, rows, width), low), hbm),
        (shape((members, 8, rows), full), vmem),
        (shape((2, width, 2 * size), low), hbm),
        (shape((2, size, width), low), hbm),
        (shape((grps, slab, both_hidden), low), hbm),
        (shape((grps, units, width), low), hbm),
    ]
    dma = pltpu.SemaphoreType.DMA
    return pl.pallas_call(
        functools.partial(expert_kernel, grps, exps, cap),
        out_shape=[r[0] for r in results],
        in_specs=[smem] + [vmem] * 2 + [hbm] * 6,
        out_specs=[r[1] for r in results],
        scratch_shapes=[
            pltpu.VMEM((members, cap, rows), low),
            pltpu.VMEM((QUAD * slots, 128), full),
            pltpu.VMEM((QUAD * slots, width), low),
            pltpu.VMEM((QUAD * slots, width), low),
            pltpu.VMEM((tiles.count, width, 2 * size), low),
            pltpu.VMEM((tiles.count, size, width), low),
            pltpu.VMEM((2, exps, rows, width), low),
            pltpu.VMEM((2, exps, rows, width), low),
            pltpu.VMEM((QUAD * slots, width), low),
            pltpu.VMEM((QUAD * slots, width), full),
            pltpu.VMEM((QUAD * slots, 2 * size), low),
            pltpu.VMEM((QUAD * slots, size), low),
            pltpu.VMEM((tiles.count, width, 2 * size), low),
            pltpu.VMEM((tiles.count, size, width), low),
            pltpu.VMEM((2, rows, width), low),
            pltpu.VMEM((2, rows, width), low),
            dma((2, 2)),
            dma((2, 2)),
            dma((2, 2)),
            dma((2, 2 * reps)),
            dma((2, reps + 1)),
            dma((2, 2 * reps)),
            dma((2, max(QUAD, grps))),
            dma((2, tiles.count)),
        ],
        compiler_params=pltpu.CompilerParams(
            collective_id=2, has_side_effects=True, vmem_limit_bytes=60 * 1024 * 1024
        ),
        name="experts",
    )(deal, routes_t, comb_all, n_all, cot_all, both_w, down_w, in_low, down_slab)


def adam_kernel(exps, *refs):
    in_parts, down_parts, qkv_grad, out_grad, small = refs[:5]
    states, news, bias_grad = refs[5:26], refs[26:47], refs[47]
    heads = HEADS // exps
    width = small.shape[1]

    def update(i, grad, rate, decay):
        weight, first, second = [state[...] for state in states[3 * i : 3 * i + 3]]
        values = adamw_update(weight, first, second, grad, rate, decay)
        for new, value in zip(news[3 * i : 3 * i + 3], values, strict=True):
            new[...] = value

    def total(parts):
        result = parts[0].astype(full)
        for k in range(1, parts.shape[0]):
            result = result + parts[k].astype(full)
        return result

    @pl.when(pl.program_id(0) == 0)
    def _():
        update(0, qkv_grad[...], 1.5 / math.sqrt(D), 0.1)
        update(1, out_grad[...], 6.0 / math.sqrt(D), 0.1)
        for e in range(exps):
            for h in range(heads):
                bias_grad[e * heads + h : e * heads + h + 1, :] = small[
                    exps + 3 + e : exps + 4 + e, h * 128 : h * 128 + BUCKETS
                ]
        update(2, bias_grad[...], 0.3, 0.0)
        update(3, small[0:exps, :], 1.0 / math.sqrt(D), 0.1)
        update(4, small[exps : exps + 2, :], 0.5, 0.0)

    update(5, total(in_parts), 1.5 / math.sqrt(D), 0.1)
    update(6, total(down_parts), 1.5 / math.sqrt(FF), 0.1)


def adam_call(exps, in_parts, down_parts, qkv_grad, out_grad, small, states):
    steps = 4

    def whole(array):
        return pl.BlockSpec(array.shape, lambda i: (0,) * array.ndim)

    def columns(array):
        block = array.shape[:-1] + (array.shape[-1] // steps,)
        return pl.BlockSpec(block, lambda i: (0,) * (array.ndim - 1) + (i,))

    specs = [whole(state) for state in states[:15]] + [columns(state) for state in states[15:]]
    return pl.pallas_call(
        functools.partial(adam_kernel, exps),
        grid=(steps,),
        in_specs=[columns(in_parts), columns(down_parts), whole(qkv_grad), whole(out_grad), whole(small)] + specs,
        out_specs=specs,
        out_shape=[jax.ShapeDtypeStruct(state.shape, full) for state in states],
        scratch_shapes=[pltpu.VMEM((HEADS, BUCKETS), full)],
        compiler_params=pltpu.CompilerParams(vmem_limit_bytes=60 * 1024 * 1024),
        name="adam",
    )(in_parts, down_parts, qkv_grad, out_grad, small, *states)


class Halving:
    def __init__(self, at, source, kept, bufs, sems, load_sem, orders):
        self.at, self.source, self.kept, self.bufs = at, source, kept, bufs
        self.sems, self.load_sem = sems, load_sem
        self.plane = at.quad * at.exps + at.exp
        self.places = bits_of(QUAD * at.exps)
        self.chip_bits = list(range(self.places - 1))
        self.parts = column_parts(source.shape[2])
        self.orders = orders

    def device(self, bit):
        other = flipped(self.plane, bit)
        return (self.at.grp, other // self.at.exps, other % self.at.exps)

    def first(self):
        core = self.plane % 2
        count = 1 << (self.places - 1)
        device = self.device(0)

        def copies(j):
            return send(
                self.source.at[2 * j + 1 - core], self.bufs[0].at[j], self.sems.at[0, 0, j], self.sems.at[0, 1, j], device
            )

        def load(j):
            return pltpu.make_async_copy(self.source.at[2 * j + core], self.kept.at[j], self.load_sem.at[j])

        return count, copies, load

    def start_first(self):
        count, copies, load = self.first()

        def one(j, _):
            copies(j).start()
            load(j).start()
            return 0

        lax.fori_loop(0, count, one, 0)

    def add_first(self):
        count, copies, load = self.first()

        def one(j, _):
            arrived(self.bufs[0].at[j], self.sems.at[0, 1, j])
            load(j).wait()
            self.bufs[0][j] = self.bufs[0][j] + self.kept[j]
            return 0

        lax.fori_loop(0, count, one, 0)

    def hop(self, step, part):
        order = self.orders[part]
        bit = order[step]
        left = [b for b in self.chip_bits if b not in order[:step]]
        pos = left.index(bit)
        half = 1 << (len(left) - 1)
        mine = (self.plane // (1 << (bit + 1))) % 2
        device = self.device(bit + 1)
        begin, size = self.parts[part]
        cols = pl.ds(begin, size)
        base = self.base(step, part)

        def index(j, value):
            return (j >> pos) * (1 << (pos + 1)) + value * (1 << pos) + j % (1 << pos)

        pairs = []
        for j in range(half):
            copy = functools.partial(
                send,
                self.bufs[step].at[index(j, 1 - mine), :, cols],
                self.bufs[step + 1].at[j, :, cols],
                self.sems.at[1, 0, base + j],
                self.sems.at[1, 1, base + j],
                device,
            )
            pairs.append((copy, index(j, mine), j))
        return pairs, begin, size, base

    def base(self, step, part):
        n = len(self.chip_bits)
        return part * (1 << n) + sum(1 << (n - 1 - s) for s in range(step))

    def start(self, step, part=None):
        for p in range(3) if part is None else [part]:
            for copy, _, _ in self.hop(step, p)[0]:
                copy().start()

    def add(self, step, part):
        pairs, begin, size, base = self.hop(step, part)
        cols = pl.ds(begin, size)
        here, there = self.bufs[step], self.bufs[step + 1]
        for _, keep, j in pairs:
            arrived(there.at[j, :, cols], self.sems.at[1, 1, base + j])
            there[j, :, begin : begin + size] = (
                there[j, :, begin : begin + size] + here[keep, :, begin : begin + size]
            )

    def next(self, step):
        for p in range(3):
            self.add(step, p)
            if step + 1 < len(self.chip_bits):
                self.start(step + 1, p)

    def result(self):
        return self.bufs[len(self.chip_bits)]

    def finish(self):
        count, copies, _ = self.first()

        def one(j, _):
            copies(j).wait_send()
            return 0

        lax.fori_loop(0, count, one, 0)
        for step in range(len(self.chip_bits)):
            for p in range(3):
                for copy, _, _ in self.hop(step, p)[0]:
                    copy().wait_send()


def backward_kernel(
    grps,
    exps,
    lengths,
    deal,
    bias_table,
    n_parts,
    y_parts,
    c_parts,
    both_g,
    down_g,
    in_before,
    down_before,
    n1_in,
    cot_all,
    routes_t,
    tokens,
    h1_in,
    n2_in,
    probs_in,
    qkv,
    lse,
    mine,
    wqkv,
    wout,
    gains,
    router_t,
    *rest,
):
    token_grad, block_out, in_parts, down_parts, qkv_grad, out_grad, small_out = rest[:7]
    scratch = rest[7:]
    (
    kept,
    n_bufs,
    y_bufs,
    c_in,
    dh1,
    dz_send,
    dz_all,
    do_send,
    do_in,
    bias,
    bias_sum,
    dqkv,
    dqkv_t,
    dn1_send,
    dn1_in,
    wq_send,
    og_send,
    mids,
    far_send,
    far_in,
    blk_send,
    blk_in,
    small_send,
    small_exp,
    small_sum,
    small_rep,
    n_sem,
    y_sem,
    load_sem,
    c_sem,
    weight_sem,
    down_sem,
    dz_sem,
    do_sem,
    dn1_sem,
    wq_sem,
    og_sem,
    mid_sem,
    far_sem,
    blk_sem,
    small_sem,
    small2_sem,
    n1_sem,
    ) = scratch
    at = Where(grps, exps)
    reps = at.reps
    rows, width = tokens.shape
    heads = HEADS // exps
    head_dim = width // HEADS
    head_cols = heads * head_dim
    block_cols = min(128, head_cols)
    row_block = wqkv.shape[2]
    out_cols = wout.shape[3]
    tiles = Tiles(down_parts.shape[1], reps)
    scale = 1.0 / math.sqrt(head_dim)
    SEND, RECV = 0, 1
    plane = at.quad * exps + at.exp
    members = QUAD * exps

    def exp_peer(k):
        return (at.exp + k) % exps

    router = router_t[...]
    n1 = kept.at[0:exps]
    group = pl.ds(pl.multiple_of(at.quad * exps, exps), exps)
    cot_copy = pltpu.make_async_copy(cot_all.at[group], dn1_send, n1_sem.at[1])
    cot_copy.start()
    greet_all(at)

    dn = Halving(at, n_parts, kept, n_bufs, n_sem, load_sem.at[0], [[0, 1, 2], [1, 2, 0], [2, 0, 1]])
    ys = Halving(at, y_parts, kept, y_bufs, y_sem, load_sem.at[1], [[1, 0, 2], [1, 0, 2], [0, 1, 2]])
    dn.start_first()
    homes = [
        Homeward(
            at, tiles, t + 1, both_g.at[t], down_g.at[t], in_parts, down_parts, weight_sem.at[t], down_sem.at[t]
        )
        for t in range(2)
    ]
    n1_copy = pltpu.make_async_copy(n1_in, n1, n1_sem.at[0])

    def c_copy(k):
        other = (plane + k) % members
        return other, send(
            c_parts.at[other],
            c_in.at[plane],
            c_sem.at[SEND, other],
            c_sem.at[RECV, plane],
            (at.grp, other // exps, other % exps),
        )

    def start_c(k, _):
        c_copy(k)[1].start()
        return 0

    lax.fori_loop(1, members, start_c, 0)
    pltpu.make_async_copy(c_parts.at[plane], c_in.at[plane], c_sem.at[RECV, plane]).start()

    span = 2 * rows
    bucket = bucket_of(lane_of((8, span)) - rows)
    for h in range(heads):
        line = jnp.zeros((8, span), full)
        for b in range(BUCKETS):
            line = jnp.where(bucket == b, bias_table[at.exp * heads + h, b], line)
        whole = jnp.broadcast_to(line[0:1], (rows, span))
        bias[h] = pltpu.roll(whole, 0, 1, stride=1, stride_axis=0)[:, rows:]

    dn.add_first()
    dn.start(0)
    ys.start_first()

    def wait_c(k, _):
        arrived(c_in.at[k], c_sem.at[RECV, k])
        return 0

    lax.fori_loop(0, members, wait_c, 0)
    lane = lane_of((rows, 128))
    comb_rows = []
    for e in range(exps):
        total = c_in[e]
        for q in range(1, QUAD):
            total = total + c_in[q * exps + e]
        comb_rows.append(total[0:1, :])
    comb_rows.append(jnp.zeros((128 - exps, rows), full))
    comb_grad = jnp.concatenate(comb_rows, axis=0).T
    valid = row_of((rows, 1)) < lengths[at.me]
    probs = probs_in[...]
    hot = routed(routes_t, at.me, rows)
    picked = jnp.where(hot, probs, 0.0)
    total = jnp.sum(picked, axis=1, keepdims=True)
    gate = picked / total
    gate_grad_rows = jnp.where(valid, comb_grad, 0.0)
    spread_grad = jnp.sum(gate_grad_rows * gate, axis=1, keepdims=True)
    probs_grad = jnp.where(hot, (gate_grad_rows - spread_grad) / total, 0.0)
    logit_grad = probs * (probs_grad - jnp.sum(probs_grad * probs, axis=1, keepdims=True))
    n2 = n2_in[...].astype(full)
    router_rows = lax.dot_general(
        logit_grad, n2, (((0,), (0,)), ((), ())), preferred_element_type=full, precision=highest
    )
    small_rows = small_send.shape[0]
    small_send[...] = jnp.zeros_like(small_send)
    small_send[0:exps, :] = router_rows[0:exps, :]
    router_back = jnp.dot(
        logit_grad, jnp.concatenate([router, jnp.zeros((128 - exps, width), full)], axis=0),
        precision=highest, preferred_element_type=full,
    )
    h1 = h1_in[...]
    r2 = lax.rsqrt(jnp.mean(h1 * h1, axis=1, keepdims=True) + eps_norm)

    dn.next(0)
    ys.add_first()
    n1_copy.start()
    dn.next(1)
    homes[0].start()
    steps = len(dn.chip_bits)
    for step in range(2, steps):
        dn.next(step)

    n2_grad = router_back + dn.result()[0].astype(full)
    scaled = n2_grad * gains[1:2, :]
    cot_copy.wait()
    dealt = deal[at.me] - at.base
    g = dn1_send[0]
    for e in range(1, exps):
        g = jnp.where(dealt == e, dn1_send[e], g)
    hidden_grad = (
        jnp.where(valid, g.astype(full), 0.0)
        + r2 * scaled
        - h1 * (r2 * r2 * r2) * jnp.mean(scaled * h1, axis=1, keepdims=True)
    )
    dh1[...] = hidden_grad
    small_send[exps + 1 : exps + 2, :] = jnp.sum(n2_grad * h1 * r2, axis=0, keepdims=True)
    branch = hidden_grad.astype(low)
    dz_send[...] = branch
    for e in range(exps):
        total = jnp.zeros((rows, row_block), full)
        for r in range(reps):
            total = total + nt(branch[:, r * out_cols : (r + 1) * out_cols], wout[e, r])
        do_send[e] = total.astype(low)

    def do_copies():
        return [
            send(
                do_send.at[exp_peer(k)],
                do_in.at[at.exp],
                do_sem.at[SEND, exp_peer(k)],
                do_sem.at[RECV, at.exp],
                at.device(at.rep, exp_peer(k)),
            )
            for k in range(1, exps)
        ]

    for copy in do_copies():
        copy.start()
    pltpu.make_async_copy(do_send.at[at.exp], do_in.at[at.exp], do_sem.at[RECV, at.exp]).start()

    group_dz = Group(at, dz_send, dz_all, dz_sem)
    group_dz.start()
    dz_all[at.exp] = branch
    ys.start(0)
    homes[1].start()

    bias_sum[...] = jnp.zeros_like(bias_sum)

    group_blk = Group(at, blk_send, blk_in, blk_sem)

    def dn1_copies():
        beside, across = turn(at.exp, 2), turn(at.exp, 1)
        return [
            functools.partial(
                send, dn1_send.at[k], dn1_in.at[j], dn1_sem.at[SEND, j], dn1_sem.at[RECV, j], at.device(at.rep, to)
            )
            for k, j, to in ((turn(at.exp, 0), 2, beside), (across, 0, across), (beside, 1, beside))
        ]

    def attend_back(i, _):
        s = turn(at.exp, i)
        @pl.when(i == 1)
        def _():
            group_dz.pass_on()

        arrived(do_in.at[s], do_sem.at[RECV, s])
        ok = lane_of((rows, rows)) < lengths[at.base + s]
        block_lane = lane_of((rows, block_cols))
        for c in range(head_cols // block_cols):
            cols = slice(c * block_cols, (c + 1) * block_cols)
            k_cols = slice(head_cols + c * block_cols, head_cols + (c + 1) * block_cols)
            v_cols = slice(2 * head_cols + c * block_cols, 2 * head_cols + (c + 1) * block_cols)
            q = qkv[s, :, cols] * scale
            k = qkv[s, :, k_cols]
            v = qkv[s, :, v_cols]
            do = do_in[s, :, cols]
            dq = jnp.zeros((rows, block_cols), full)
            dk = jnp.zeros((rows, block_cols), full)
            dv = jnp.zeros((rows, block_cols), full)
            for t in range(block_cols // head_dim):
                h = c * (block_cols // head_dim) + t
                here = jnp.logical_and(block_lane >= t * head_dim, block_lane < (t + 1) * head_dim)
                zero = jnp.zeros_like(q)
                q_h = jnp.where(here, q, zero)
                do_h = jnp.where(here, do, zero)
                scores = nt(q_h, k) + bias[h]
                p = jnp.where(ok, jnp.exp(scores - lse[s, :, h : h + 1]), 0.0)
                dp = nt(do_h, v)
                delta = jnp.sum(dp * p, axis=1, keepdims=True)
                ds = (p * (dp - delta)).astype(low)
                bias_sum[h] += ds.astype(full)
                dv = jnp.where(here, tn(p.astype(low), do), dv)
                dq = jnp.where(here, jnp.dot(ds, k, preferred_element_type=full), dq)
                dk = jnp.where(here, tn(ds, q), dk)
            dqkv[:, cols] = (dq * scale).astype(low)
            dqkv[:, k_cols] = dk.astype(low)
            dqkv[:, v_cols] = dv.astype(low)
        dqkv_t[:, pl.ds(pl.multiple_of(s * rows, rows), rows)] = dqkv[...].T
        for e in range(exps):
            dn1_send[s, :, e * row_block : (e + 1) * row_block] = jnp.dot(
                dqkv[...], wqkv[e], preferred_element_type=full
            ).astype(low)

        @pl.when(i == 0)
        def _():
            dn1_copies()[0]().start()

        @pl.when(i == 1)
        def _():
            arrived(dn1_in.at[2], dn1_sem.at[RECV, 2])
            dn1_send[s] = (dn1_send[s].astype(full) + dn1_in[2].astype(full)).astype(low)
            dn1_copies()[1]().start()

        @pl.when(i == 2)
        def _():
            dn1_copies()[2]().start()

        return 0

    lax.fori_loop(0, exps, attend_back, 0)

    n1_copy.wait()
    seg = wq_send.shape[2]
    parts = wq_send.shape[1]
    segs = mids.shape[1] - 1
    for e in range(exps):
        part = kept[0:exps, :, e * row_block : (e + 1) * row_block].reshape(exps * rows, row_block)
        total = dot(dqkv_t[...], part)
        for j in range(parts):
            wq_send[e, j] = total[j * seg : (j + 1) * seg].astype(low)

    def owner(j):
        section, within = j // (head_cols // seg), j % (head_cols // seg)
        col = section * width + at.exp * head_cols + within * seg
        block = col // seg
        return block // segs, block % segs

    def mid_place(grp, k, quad):
        return (grp * (segs + 1) + k) * QUAD + quad

    def mid_copy(src, send_sem, rep, k, e):
        dst = mids.at[rep // QUAD, k, at.quad]
        recv = mid_sem.at[mid_place(rep // QUAD, k, at.quad)]
        stays = jnp.logical_and(rep % QUAD == at.quad, e == at.exp)
        return (
            stays,
            functools.partial(send, src, dst, send_sem, recv, (at.grp, rep % QUAD, e)),
            functools.partial(pltpu.make_async_copy, src, dst, recv),
        )

    def wq_copy(i):
        e, j = i // parts, i % parts
        rep, k = owner(j)
        return mid_copy(wq_send.at[e, j], wq_sem.at[i], rep, k, e)

    def og_copy(r):
        return mid_copy(og_send.at[r], og_sem.at[r], r, segs, at.exp)

    def go(copies, act, act_local):
        stays, away, local = copies

        @pl.when(jnp.logical_not(stays))
        def _():
            act(away)

        if act_local:

            @pl.when(stays)
            def _():
                act_local(local)

    def over(count, copies, act, act_local):
        def one(i, _):
            go(copies(i), act, act_local)
            return 0

        lax.fori_loop(0, count, one, 0)

    over(exps * parts, wq_copy, lambda copy: copy().start(), lambda copy: copy().start())
    group_dz.arrive()
    grad = tn(mine[...].reshape(exps * rows, head_cols), dz_all[...].reshape(exps * rows, width))
    for r in range(reps):
        og_send[r] = grad[:, r * out_cols : (r + 1) * out_cols].T.astype(low)
    over(reps, og_copy, lambda copy: copy().start(), lambda copy: copy().start())

    n1_grad = dn1_send[at.exp].astype(full)
    for j in range(2):
        arrived(dn1_in.at[j], dn1_sem.at[RECV, j])
        n1_grad = n1_grad + dn1_in[j].astype(full)
    x = tokens[...].astype(full)
    r1 = lax.rsqrt(jnp.mean(x * x, axis=1, keepdims=True) + eps_norm)
    scaled = n1_grad * gains[0:1, :]
    token_grad[...] = (
        dh1[...] + r1 * scaled - x * (r1 * r1 * r1) * jnp.mean(scaled * x, axis=1, keepdims=True)
    )
    small_send[exps : exps + 1, :] = jnp.sum(n1_grad * x * r1, axis=0, keepdims=True)

    line_lane = lane_of((8, 128))
    line_row = row_of((8, 128))
    bias_line = jnp.zeros((8, 128), full)
    flip = jnp.where(row_of((rows, rows)) + lane_of((rows, rows)) == rows - 1, 1.0, 0.0).astype(low)
    turned_bucket = bucket_of(rows - 1 - lane_of((8, span)))
    for h in range(heads):
        high = bias_sum[h].astype(low)
        rest = (bias_sum[h] - high.astype(full)).astype(low)
        flipped = dot(high, flip) + dot(rest, flip)
        square = jnp.concatenate([flipped, jnp.zeros((rows, rows), full)], axis=1)
        turned = pltpu.roll(square, 0, 1, stride=1, stride_axis=0)
        sums = jnp.broadcast_to(jnp.sum(turned, axis=0, keepdims=True), (8, span))
        for b in range(BUCKETS):
            value = jnp.sum(jnp.where(turned_bucket == b, sums, 0.0), axis=1, keepdims=True)
            bias_line = jnp.where(jnp.logical_and(line_row == h, line_lane == b), value, bias_line)
    for h in range(heads):
        small_send[exps + 2 : exps + 3, h * 128 : (h + 1) * 128] = bias_line[h : h + 1, :]

    def small_copies():
        return [
            send(
                small_send,
                small_exp.at[at.exp],
                small_sem.at[SEND, exp_peer(k)],
                small_sem.at[RECV, at.exp],
                at.device(at.rep, exp_peer(k)),
            )
            for k in range(1, exps)
        ]

    for copy in small_copies():
        copy.start()
    small_exp[at.exp] = small_send[...]
    ys.next(0)

    def mid_sum(grp, k):
        for q in range(QUAD):
            arrived(mids.at[grp, k, q], mid_sem.at[mid_place(grp, k, q)])
        total = mids[grp, k, 0].astype(full)
        for q in range(1, QUAD):
            total = total + mids[grp, k, q].astype(full)
        return total

    far = 1 - at.grp
    for k in range(segs + 1):
        far_send[k] = mid_sum(far, k).astype(low)

    def far_copy():
        return send(far_send, far_in, far_sem.at[SEND], far_sem.at[RECV], (far, at.quad, at.exp))

    far_copy().start()
    ys.next(1)
    for k in range(1, exps):
        arrived(small_exp.at[exp_peer(k)], small_sem.at[RECV, exp_peer(k)])
    total = small_exp[0]
    for e in range(1, exps):
        total = total + small_exp[e]
    small_sum[0] = total
    for e in range(exps):
        small_sum[0, exps + 3 + e : exps + 4 + e, :] = small_exp[e, exps + 2 : exps + 3, :]

    def small2_copies():
        return [
            send(
                small_sum.at[0],
                small_rep.at[at.rep],
                small2_sem.at[SEND, (at.rep + k) % reps],
                small2_sem.at[RECV, at.rep],
                at.device((at.rep + k) % reps, at.exp),
            )
            for k in range(1, reps)
        ]

    for copy in small2_copies():
        copy.start()
    small_rep[at.rep] = small_sum[0]
    for step in range(2, steps):
        ys.next(step)
    block = jnp.where(valid, h1_in[...] + ys.result()[0].astype(full), 0.0).astype(low)
    blk_send[...] = block
    group_blk.start()
    blk_in[at.exp] = block
    group_blk.pass_on()
    group_blk.arrive()
    chosen = jnp.zeros((rows, width), full)
    for e in range(exps):
        chosen = jnp.where(deal[at.base + e] == at.me, blk_in[e].astype(full), chosen)
    block_out[...] = chosen.astype(low)
    for k in range(1, reps):
        arrived(small_rep.at[(at.rep + k) % reps], small2_sem.at[RECV, (at.rep + k) % reps])
    total = small_rep[0]
    for r in range(1, reps):
        total = total + small_rep[r]
    small_out[...] = total

    near = [mid_sum(at.grp, k) for k in range(segs + 1)]
    arrived(far_in, far_sem.at[RECV])
    grads = [(near[k] + far_in[k].astype(full)).T for k in range(segs + 1)]
    qkv_grad[...] = jnp.concatenate(grads[:segs], axis=1)
    out_grad[...] = grads[segs]
    for home in homes:
        home.arrive()

    def sent_c(k, _):
        c_copy(k)[1].wait_send()
        return 0

    lax.fori_loop(1, members, sent_c, 0)
    dn.finish()
    ys.finish()

    for home in homes:
        home.sent()

    over(exps * parts, wq_copy, lambda copy: copy().wait_send(), None)
    over(reps, og_copy, lambda copy: copy().wait_send(), None)
    far_copy().wait_send()
    for copies in (do_copies(), small_copies(), small2_copies()):
        for copy in copies:
            copy.wait_send()
    for copy in dn1_copies():
        copy().wait_send()
    group_dz.sent()
    group_blk.sent()


def routed(routes_t, seq, rows):
    pair = routes_t[:, pl.ds(pl.multiple_of(seq * rows, rows), rows)].astype(full)
    cols = jnp.concatenate([pair, jnp.zeros((126, rows), full)], axis=0).T
    lane = lane_of((rows, 128)).astype(full)
    return jnp.logical_or(lane == cols[:, 0:1], lane == cols[:, 1:2])


def backward_call(
    grps, exps, lengths, deal, bias_table, n_parts, y_parts, c_parts, both_g, down_g, in_before, down_before, n1,
    cot_all, routes_t, tokens, h1, n2, probs, qkv, lse, mine, wqkv, wout, gains, router
):
    reps = grps * QUAD
    rows, width = tokens.shape
    heads = HEADS // exps
    head_cols = width // exps
    row_block = wqkv.shape[2]
    out_cols = wout.shape[3]
    shard_cols = 3 * width // reps
    seg = math.gcd(shard_cols, head_cols)
    segs = shard_cols // seg
    parts = 3 * head_cols // seg
    members = QUAD * exps
    chip_bits = bits_of(members) - 1
    small_rows = -(-(2 * exps + 3) // 8) * 8
    shape = jax.ShapeDtypeStruct
    vmem = pl.BlockSpec(memory_space=pltpu.VMEM)
    smem = pl.BlockSpec(memory_space=pltpu.SMEM)
    hbm = pl.BlockSpec(memory_space=pl.ANY)
    results = [
        (shape((rows, width), full), vmem),
        (shape((rows, width), low), vmem),
        (shape(in_before.shape, low), hbm),
        (shape(down_before.shape, low), hbm),
        (shape((row_block, shard_cols), full), vmem),
        (shape((row_block, out_cols), full), vmem),
        (shape((small_rows, width), full), vmem),
    ]
    dma = pltpu.SemaphoreType.DMA
    bufs = [pltpu.VMEM((1 << (chip_bits - s), rows, width), low) for s in range(chip_bits + 1)]
    return pl.pallas_call(
        functools.partial(backward_kernel, grps, exps),
        out_shape=[r[0] for r in results],
        in_specs=[smem] * 3 + [hbm] * 9 + [vmem] * 12,
        out_specs=[r[1] for r in results],
        scratch_shapes=[
            pltpu.VMEM((members // 2, rows, width), low),
            list(bufs),
            list(bufs),
            pltpu.VMEM((members, 8, rows), full),
            pltpu.VMEM((rows, width), full),
            pltpu.VMEM((rows, width), low),
            pltpu.VMEM((exps, rows, width), low),
            pltpu.VMEM((exps, rows, head_cols), low),
            pltpu.VMEM((exps, rows, head_cols), low),
            pltpu.VMEM((heads, rows, rows), full),
            pltpu.VMEM((heads, rows, rows), full),
            pltpu.VMEM((rows, 3 * head_cols), low),
            pltpu.VMEM((3 * head_cols, exps * rows), low),
            pltpu.VMEM((exps, rows, width), low),
            pltpu.VMEM((3, rows, width), low),
            pltpu.VMEM((exps, parts, seg, row_block), low),
            pltpu.VMEM((reps, seg, row_block), low),
            pltpu.VMEM((grps, segs + 1, QUAD, seg, row_block), low),
            pltpu.VMEM((segs + 1, seg, row_block), low),
            pltpu.VMEM((segs + 1, seg, row_block), low),
            pltpu.VMEM((rows, width), low),
            pltpu.VMEM((exps, rows, width), low),
            pltpu.VMEM((small_rows, width), full),
            pltpu.VMEM((exps, small_rows, width), full),
            pltpu.VMEM((1, small_rows, width), full),
            pltpu.VMEM((reps, small_rows, width), full),
            dma((2, 2, 3 << chip_bits)),
            dma((2, 2, 3 << chip_bits)),
            dma((2, members // 2)),
            dma((2, members)),
            dma((2, 2, 2 * reps)),
            dma((2, 2, max(QUAD, grps))),
            dma((2, exps)),
            dma((2, exps)),
            dma((2, exps)),
            dma((exps * parts,)),
            dma((reps,)),
            dma((grps * (segs + 1) * QUAD,)),
            dma((2,)),
            dma((2, exps)),
            dma((2, exps)),
            dma((2, reps)),
            dma((2,)),
        ],
        compiler_params=pltpu.CompilerParams(
            collective_id=1, has_side_effects=True, vmem_limit_bytes=60 * 1024 * 1024
        ),
        input_output_aliases={8: 2, 9: 3},
        name="backward",
    )(
        lengths, deal, bias_table, n_parts, y_parts, c_parts, both_g, down_g, in_before, down_before, n1, cot_all,
        routes_t, tokens, h1, n2, probs, qkv, lse, mine, wqkv, wout, gains, router
    )


def per_device(
    tokens,
    cotangent,
    seq_lengths,
    deal,
    routes,
    attn_qkv,
    qkv_first,
    qkv_second,
    attn_out,
    out_first,
    out_second,
    rel_bias,
    bias_first,
    bias_second,
    router,
    router_first,
    router_second,
    norm_gains,
    gains_first,
    gains_second,
    expert_in,
    in_first,
    in_second,
    expert_out,
    down_first,
    down_second,
):
    rows, width = tokens.shape
    experts = router.shape[1]
    capacity = (10 * rows + 4 * experts - 1) // (4 * experts)
    exps = lax.axis_size("exp")
    grps = lax.axis_size("grp")
    in_low = expert_in[0].astype(low)
    down_low = expert_out[0].astype(low)
    routes_t = routes.T
    bias_table = rel_bias.T
    (
        both_w, down_w, cot_all, n_all, comb_all, qkv, lse, context_mine, normed_group, wqkv, wout, hidden_one,
        normed_two, router_probs,
    ) = forward_call(
        grps, exps, seq_lengths, bias_table, routes_t, tokens, cotangent, norm_gains.T, router.T,
        attn_qkv.astype(low).T, attn_out.astype(low), in_low, down_low,
    )
    n_parts, y_parts, c_parts, both_g, down_g, in_before, down_before = expert_call(
        grps, exps, capacity, deal, routes_t, comb_all, n_all, cot_all, both_w, down_w, in_low, down_low
    )
    token_grad, block_out, in_parts, down_parts, qkv_grad, out_grad, small = backward_call(
        grps, exps, seq_lengths, deal, bias_table, n_parts, y_parts, c_parts, both_g, down_g, in_before, down_before,
        normed_group, cot_all, routes_t, tokens, hidden_one, normed_two, router_probs, qkv, lse, context_mine, wqkv,
        wout, norm_gains.T, router.T,
    )
    states = [
        attn_qkv, qkv_first, qkv_second, attn_out, out_first, out_second, bias_table, bias_first.T, bias_second.T,
        router.T, router_first.T, router_second.T, norm_gains.T, gains_first.T, gains_second.T,
        expert_in[0], in_first[0], in_second[0], expert_out[0], down_first[0], down_second[0],
    ]
    new = list(adam_call(exps, in_parts, down_parts, qkv_grad, out_grad, small, states))
    new = new[:6] + [array.T for array in new[6:15]] + [array[None] for array in new[15:]]
    return (block_out, token_grad, *new)


def bucket_onehot(length):
    places = jnp.arange(length, dtype=jnp.int32)
    offset = places[None, :] - places[:, None]
    distance = jnp.abs(offset)
    bucket = 16 * (offset > 0).astype(jnp.int32)
    for threshold in thresholds:
        bucket = bucket + (distance >= threshold).astype(jnp.int32)
    return (bucket[:, :, None] == jnp.arange(BUCKETS, dtype=jnp.int32)[None, None, :]).astype(full)


def swap(pieces, axes):
    return lax.all_to_all(pieces, axes, split_axis=0, concat_axis=0, tiled=True)


def spread(block, axes):
    members = lax.axis_size(axes)
    return swap(jnp.broadcast_to(block[None], (members,) + block.shape), axes)


def plain_device(
    tokens,
    cotangent,
    seq_lengths,
    deal,
    routes,
    attn_qkv,
    qkv_first,
    qkv_second,
    attn_out,
    out_first,
    out_second,
    rel_bias,
    bias_first,
    bias_second,
    router,
    router_first,
    router_second,
    norm_gains,
    gains_first,
    gains_second,
    expert_in,
    in_first,
    in_second,
    expert_out,
    down_first,
    down_second,
):
    rows, width = tokens.shape
    head_dim = width // HEADS
    score_scale = 1.0 / math.sqrt(head_dim)
    experts = router.shape[1]
    capacity = (10 * rows + 4 * experts - 1) // (4 * experts)
    exps = lax.axis_size("exp")
    grps = lax.axis_size("grp")
    reps = grps * QUAD
    heads = HEADS // exps
    head_cols = heads * head_dim
    place = lax.axis_index("exp")
    base = lax.axis_index(REP) * exps
    me = base + place
    slab = expert_in.shape[1]
    units = expert_out.shape[1]
    quarter = grps * units

    row_block = attn_qkv.shape[0]
    qkv_rows = lax.all_gather(attn_qkv.astype(low), REP, axis=1, tiled=True)
    out_rows = lax.all_gather(attn_out.astype(low), REP, axis=1, tiled=True)
    qkv_pieces = jnp.transpose(
        qkv_rows.reshape(row_block, 3, exps, head_cols), (2, 0, 1, 3)
    ).reshape(exps, row_block, 3 * head_cols)
    qkv_mine = swap(qkv_pieces, "exp").reshape(width, 3 * head_cols)
    full_out = spread(out_rows, "exp").reshape(width, width)

    group_tokens = spread(tokens, "exp")
    group_cotangent = spread(cotangent, "exp")
    my_cotangent = lax.dynamic_index_in_dim(group_cotangent, deal[me] - base, 0, keepdims=False)

    my_routes = lax.dynamic_slice_in_dim(routes, me * rows, rows, 0)
    places = jnp.arange(rows, dtype=jnp.int32)
    valid_rows = (places < seq_lengths[me]).astype(full)
    group_lengths = lax.dynamic_slice_in_dim(seq_lengths, base, exps, 0)
    key_ok = places[None, :] < group_lengths[:, None]
    gain_one = norm_gains[:, 0]
    gain_two = norm_gains[:, 1]

    chosen = (my_routes[:, :, None] == jnp.arange(experts, dtype=jnp.int32)[None, None, :]).astype(full)
    flat_routes = my_routes.reshape(-1)
    route_hot = (flat_routes[:, None] == jnp.arange(experts, dtype=jnp.int32)[None, :]).astype(jnp.int32)
    before = jnp.cumsum(route_hot, axis=0) - route_hot
    slot_index = jnp.sum(before * route_hot, axis=-1)
    target = (flat_routes * capacity + slot_index).reshape(rows, 2)
    slots = experts * capacity
    slot_ids = jnp.arange(slots, dtype=jnp.int32)
    place_first = slot_ids[:, None] == target[None, :, 0]
    place_second = slot_ids[:, None] == target[None, :, 1]
    place_any = jnp.logical_or(place_first, place_second).astype(low)

    shard_in = expert_in[0].astype(low).reshape(slab, 2, grps, QUAD, units)
    in_pieces = jnp.transpose(shard_in, (1, 3, 0, 2, 4)).reshape(2, 1, QUAD, slab, quarter)
    in_pieces = jnp.broadcast_to(in_pieces, (2, grps, QUAD, slab, quarter)).reshape(
        2, reps, slab, quarter
    )
    down_mine = spread(expert_out[0].astype(low), "grp").reshape(quarter, width)
    gate_mine = swap(in_pieces[0], REP).reshape(width, quarter)
    up_mine = swap(in_pieces[1], REP).reshape(width, quarter)

    upstream = my_cotangent.astype(full) * valid_rows[:, None]

    def to_experts(block):
        sent = block.reshape((1, experts) + block.shape[1:])
        sent = jnp.broadcast_to(sent, (QUAD,) + sent.shape[1:])
        return swap(sent.reshape((QUAD * experts,) + block.shape[1:]), PLANE)

    def dispatch(values):
        return dot(place_any, values).astype(low).reshape(experts, capacity, width)

    expert_upstream = to_experts(dispatch(upstream.astype(low))).reshape(-1, width)
    active_grad_bare = lax.dot_general(
        expert_upstream, down_mine, (((1,), (1,)), ((), ())), preferred_element_type=full
    )

    x_group = group_tokens.astype(full)
    scale_group = lax.rsqrt(jnp.mean(x_group * x_group, axis=-1, keepdims=True) + eps_norm)
    normed_group = (x_group * scale_group * gain_one).astype(low).reshape(exps * rows, width)
    qkv = dot(normed_group, qkv_mine).astype(low).reshape(exps, rows, 3, heads, head_dim)
    queries = qkv[:, :, 0]
    key_rows = qkv[:, :, 1]
    values = qkv[:, :, 2]
    onehot = bucket_onehot(rows)
    bias_mine = lax.dynamic_slice_in_dim(rel_bias, place * heads, heads, 1)
    bias_table = jnp.einsum("ijb,bh->hij", onehot, bias_mine, precision=highest)

    def scores_of():
        raw = (
            jnp.einsum("sihd,sjhd->shij", queries, key_rows, preferred_element_type=full)
            * score_scale
            + bias_table[None]
        )
        return jnp.where(key_ok[:, None, None, :], raw, -1e30)

    scores = scores_of()
    row_max = jnp.max(scores, axis=-1, keepdims=True)
    log_total = row_max + jnp.log(jnp.sum(jnp.exp(scores - row_max), axis=-1, keepdims=True))
    weights_low = jnp.exp(scores - log_total).astype(low)
    context_mine = (
        jnp.einsum("shij,sjhd->sihd", weights_low, values, preferred_element_type=full)
        .astype(low)
        .reshape(exps, rows, head_cols)
    )
    context = jnp.transpose(swap(context_mine, "exp"), (1, 0, 2)).reshape(rows, width)

    x_float = tokens.astype(full)
    scale_one = lax.rsqrt(jnp.mean(x_float * x_float, axis=-1, keepdims=True) + eps_norm)
    hidden_one = x_float + dot(context, full_out)
    scale_two = lax.rsqrt(jnp.mean(hidden_one * hidden_one, axis=-1, keepdims=True) + eps_norm)
    normed_two = (hidden_one * scale_two * gain_two).astype(low)
    normed_float = normed_two.astype(full)
    router_probs = jax.nn.softmax(jnp.dot(normed_float, router, precision=highest), axis=-1)
    picked = jnp.sum(router_probs[:, None, :] * chosen, axis=-1)
    gate_total = jnp.sum(picked, axis=-1, keepdims=True)
    gate_value = picked / gate_total
    combine = gate_value * valid_rows[:, None]
    combine_slots = jnp.sum(
        jnp.where(place_first, combine[None, :, 0], 0.0)
        + jnp.where(place_second, combine[None, :, 1], 0.0),
        axis=1,
    ).reshape(experts, 1, capacity)

    expert_rows = to_experts(dispatch(normed_two)).reshape(-1, width)
    expert_combine = to_experts(combine_slots).reshape(-1, 1)

    gate_part = dot(expert_rows, gate_mine)
    up_part = dot(expert_rows, up_mine)
    active_float, active_pull = jax.vjp(gated_unit, gate_part, up_part)
    active = active_float.astype(low)
    active_scaled = (active_float * expert_combine).astype(low)
    combine_grad_part = jnp.sum(active_float * active_grad_bare, axis=-1).reshape(
        QUAD * experts, 1, capacity
    )
    gate_part_grad, up_part_grad = active_pull(active_grad_bare * expert_combine)
    gate_part_grad = gate_part_grad.astype(low)
    up_part_grad = up_part_grad.astype(low)
    rows_grad_part = (
        lax.dot_general(gate_part_grad, gate_mine, (((1,), (1,)), ((), ())), preferred_element_type=full)
        + lax.dot_general(up_part_grad, up_mine, (((1,), (1,)), ((), ())), preferred_element_type=full)
    ).astype(low)
    output_part = dot(active, down_mine).astype(low)

    combine_grad_back = swap(combine_grad_part, PLANE)
    rows_grad_back = swap(rows_grad_part.reshape(QUAD * experts, capacity, width), PLANE)
    output_back = swap(output_part.reshape(QUAD * experts, capacity, width), PLANE)

    def transposed_dot(a, b):
        return lax.dot_general(a, b, (((0,), (0,)), ((), ())), preferred_element_type=full)

    down_grad = transposed_dot(active_scaled, expert_upstream).astype(low)
    gate_grad = transposed_dot(expert_rows, gate_part_grad).astype(low)
    up_grad = transposed_dot(expert_rows, up_part_grad).astype(low)
    down_share = jnp.sum(
        swap(down_grad.reshape(grps, units, width), "grp").astype(full), axis=0
    )[None]

    def in_columns(grad):
        back = swap(grad.reshape(reps, slab, quarter), REP).astype(full)
        back = jnp.sum(back.reshape(grps, QUAD, slab, grps, units), axis=0)
        return jnp.transpose(back, (1, 2, 0, 3)).reshape(slab, grps * QUAD * units)

    in_share = jnp.concatenate([in_columns(gate_grad), in_columns(up_grad)], axis=1)[None]

    def from_slots(placed, parts):
        hot = jnp.broadcast_to(placed.astype(low)[None], (QUAD,) + placed.shape).reshape(-1, rows)
        return lax.dot_general(
            hot, parts.reshape(-1, width), (((0,), (0,)), ((), ())), preferred_element_type=full
        )

    mixture = combine[:, :1] * from_slots(place_first, output_back) + combine[:, 1:] * from_slots(
        place_second, output_back
    )
    block_loader = (valid_rows[:, None] * (hidden_one + mixture)).astype(low)
    seq_ids = jnp.arange(deal.shape[0], dtype=jnp.int32)
    dealt_seq = jnp.sum(jnp.where(deal == me, seq_ids, 0))
    block_out = lax.dynamic_index_in_dim(
        spread(block_loader, "exp"), dealt_seq - base, 0, keepdims=False
    )

    combine_grad_slots = jnp.sum(combine_grad_back.reshape(QUAD, slots), axis=0)
    combine_grad = jnp.stack(
        [
            jnp.sum(jnp.where(place_first, combine_grad_slots[:, None], 0.0), axis=0),
            jnp.sum(jnp.where(place_second, combine_grad_slots[:, None], 0.0), axis=0),
        ],
        axis=1,
    )
    gate_grad_value = combine_grad * valid_rows[:, None]
    picked_grad = (
        gate_grad_value - jnp.sum(gate_grad_value * gate_value, axis=-1, keepdims=True)
    ) / gate_total
    probs_grad = jnp.sum(picked_grad[:, :, None] * chosen, axis=1)
    logit_grad = router_probs * (
        probs_grad - jnp.sum(probs_grad * router_probs, axis=-1, keepdims=True)
    )
    router_grad = jnp.dot(normed_float.T, logit_grad, precision=highest)
    normed_grad = jnp.dot(logit_grad, router.T, precision=highest) + from_slots(
        jnp.logical_or(place_first, place_second), rows_grad_back
    )
    scaled_two = normed_grad * gain_two
    hidden_grad = (
        upstream
        + scale_two * scaled_two
        - hidden_one * scale_two**3 * jnp.mean(scaled_two * hidden_one, axis=-1, keepdims=True)
    )
    gain_two_grad = jnp.sum(normed_grad * hidden_one * scale_two, axis=0)
    branch_grad = hidden_grad.astype(low)
    context_grad = lax.dot_general(
        branch_grad, full_out, (((1,), (1,)), ((), ())), preferred_element_type=full
    ).astype(low)
    context_grad_pieces = jnp.transpose(context_grad.reshape(rows, exps, head_cols), (1, 0, 2))
    context_grad_mine = swap(context_grad_pieces, "exp").reshape(exps, rows, heads, head_dim)
    branch_group = spread(branch_grad, "exp").reshape(exps * rows, width)
    out_grad = transposed_dot(context_mine.reshape(exps * rows, head_cols), branch_group).astype(low)

    scores = scores_of()
    probs_again = jnp.exp(scores - log_total)
    weights_again = probs_again.astype(low)
    values_grad = jnp.einsum(
        "shij,sihd->sjhd", weights_again, context_grad_mine, preferred_element_type=full
    )
    probs_grad_att = jnp.einsum(
        "sihd,sjhd->shij", context_grad_mine, values, preferred_element_type=full
    )
    row_delta = jnp.sum(probs_grad_att * probs_again, axis=-1, keepdims=True)
    scores_grad = (probs_again * (probs_grad_att - row_delta)).astype(low)
    scores_grad_sum = jnp.sum(scores_grad.astype(full), axis=0)
    bias_grad_mine = jnp.einsum("hij,ijb->bh", scores_grad_sum, onehot, precision=highest)
    bias_grad = lax.dynamic_update_slice_in_dim(
        jnp.zeros((BUCKETS, HEADS), full), bias_grad_mine, place * heads, 1
    )
    queries_grad = (
        jnp.einsum("shij,sjhd->sihd", scores_grad, key_rows, preferred_element_type=full)
        * score_scale
    )
    keys_grad = (
        jnp.einsum("shij,sihd->sjhd", scores_grad, queries, preferred_element_type=full)
        * score_scale
    )
    qkv_grad = (
        jnp.stack([queries_grad, keys_grad, values_grad], axis=2)
        .astype(low)
        .reshape(exps * rows, 3 * head_cols)
    )
    normed_one_part = lax.dot_general(
        qkv_grad, qkv_mine, (((1,), (1,)), ((), ())), preferred_element_type=full
    ).astype(low)
    normed_one_grad = jnp.sum(
        swap(normed_one_part.reshape(exps, rows, width), "exp").astype(full), axis=0
    )
    scaled_one = normed_one_grad * gain_one
    token_grad = (
        hidden_grad
        + scale_one * scaled_one
        - x_float * scale_one**3 * jnp.mean(scaled_one * x_float, axis=-1, keepdims=True)
    )
    gain_one_grad = jnp.sum(normed_one_grad * x_float * scale_one, axis=0)

    qkv_weight_grad = transposed_dot(normed_group, qkv_grad).astype(low)
    qkv_grad_rows = swap(qkv_weight_grad.reshape(exps, row_block, 3 * head_cols), "exp")
    qkv_grad_rows = jnp.transpose(
        qkv_grad_rows.reshape(exps, row_block, 3, head_cols), (1, 2, 0, 3)
    ).reshape(row_block, reps, -1)
    qkv_share = jnp.sum(
        swap(jnp.transpose(qkv_grad_rows, (1, 0, 2)), REP).astype(full), axis=0
    )
    out_pieces = jnp.transpose(out_grad.reshape(row_block, reps, -1), (1, 0, 2))
    out_share = jnp.sum(swap(out_pieces, REP).astype(full), axis=0)

    small = jnp.concatenate(
        [
            router_grad.reshape(-1),
            jnp.stack([gain_one_grad, gain_two_grad], axis=1).reshape(-1),
            bias_grad.reshape(-1),
        ]
    ).reshape(-1, 128)
    small_total = jnp.sum(lax.all_gather(small, ALL, axis=0, tiled=False), axis=0).reshape(-1)
    router_total = small_total[: router.size].reshape(router.shape)
    gains_total = small_total[router.size : router.size + norm_gains.size].reshape(norm_gains.shape)
    bias_total = small_total[router.size + norm_gains.size :].reshape(rel_bias.shape)

    qkv_new = adamw_update(attn_qkv, qkv_first, qkv_second, qkv_share, 1.5 / math.sqrt(D), 0.1)
    out_new = adamw_update(attn_out, out_first, out_second, out_share, 6.0 / math.sqrt(D), 0.1)
    bias_new = adamw_update(rel_bias, bias_first, bias_second, bias_total, 0.3, 0.0)
    router_new = adamw_update(
        router, router_first, router_second, router_total, 1.0 / math.sqrt(D), 0.1
    )
    gains_new = adamw_update(norm_gains, gains_first, gains_second, gains_total, 0.5, 0.0)
    in_new = adamw_update(expert_in, in_first, in_second, in_share, 1.5 / math.sqrt(D), 0.1)
    down_new = adamw_update(
        expert_out, down_first, down_second, down_share, 1.5 / math.sqrt(FF), 0.1
    )
    return (
        (block_out, token_grad)
        + qkv_new
        + out_new
        + bias_new
        + router_new
        + gains_new
        + in_new
        + down_new
    )


def solution(mesh):
    reps, exps = mesh.devices.shape
    split = Mesh(mesh.devices.reshape(reps // QUAD, QUAD, exps), ALL)
    by_rows = P(ALL, None)
    attn = P("exp", REP)
    expert = P("exp", REP, None)
    return jax.shard_map(
        per_device if (reps, exps) == (2 * QUAD, 4) else plain_device,
        mesh=split,
        in_specs=(by_rows, by_rows) + (P(),) * 3 + (attn,) * 6 + (P(),) * 9 + (expert,) * 6,
        out_specs=(by_rows, by_rows) + (attn,) * 6 + (P(),) * 9 + (expert,) * 6,
        check_vma=False,
    )
```

```python
import functools
import math

import jax
import jax.numpy as jnp
from jax import lax
from jax.experimental import pallas as pl
from jax.experimental.pallas import tpu as pltpu
from jax.sharding import Mesh
from jax.sharding import PartitionSpec as P

D = 1024
HEADS = 16
FF = 2816
BUCKETS = 32
STEP = 10
QUAD = 4
REP = ("grp", "quad")
PLANE = ("quad", "exp")
ALL = ("grp", "quad", "exp")

highest = lax.Precision.HIGHEST
eps_norm = 1e-06
thresholds = (1, 2, 3, 4, 5, 6, 7, 8, 11, 16, 22, 32, 45, 64, 90)
beta_one = 0.9
beta_two = 0.999
eps_adam = 1e-08
low = jnp.bfloat16
full = jnp.float32
MESH = pl.DeviceIdType.MESH


def adamw_update(weight, moment, second, gradient, step_rate, decay_factor):
    new_moment = beta_one * moment + (1.0 - beta_one) * gradient
    new_second = beta_two * second + (1.0 - beta_two) * gradient * gradient
    corrected = new_moment / (1.0 - beta_one**STEP)
    scaled = new_second / (1.0 - beta_two**STEP)
    new_weight = weight - step_rate * (
        corrected / (jnp.sqrt(scaled) + eps_adam) + decay_factor * weight
    )
    return (new_moment, new_second, new_weight)


def gated_unit(gate_input, up_input):
    return jax.nn.gelu(gate_input, approximate=True) * up_input


def dot(a, b):
    return jnp.dot(a, b, preferred_element_type=full)


def nt(a, b, precision=None):
    return lax.dot_general(a, b, (((1,), (1,)), ((), ())), preferred_element_type=full, precision=precision)


def tn(a, b):
    return lax.dot_general(a, b, (((0,), (0,)), ((), ())), preferred_element_type=full)


class Where:
    def __init__(self, grps, exps):
        self.grps, self.exps = grps, exps
        self.reps = grps * QUAD
        self.grp = lax.axis_index("grp")
        self.quad = lax.axis_index("quad")
        self.exp = lax.axis_index("exp")
        self.rep = self.grp * QUAD + self.quad
        self.base = self.rep * exps
        self.me = self.base + self.exp

    def device(self, rep, exp):
        return (rep // QUAD, rep % QUAD, exp)

    def near(self, flip):
        q = self.quad
        if flip & 1:
            q = q + 1 - 2 * (q % 2)
        if flip & 2:
            q = q + 2 - 4 * (q // 2)
        return q


def send(src, dst, send_sem, recv_sem, device):
    return pltpu.make_async_remote_copy(
        src_ref=src, dst_ref=dst, send_sem=send_sem, recv_sem=recv_sem, device_id=device, device_id_type=MESH
    )


def arrived(ref, sem):
    pltpu.make_async_copy(ref, ref, sem).wait()


def greet(at, count, device):
    barrier = pltpu.get_barrier_semaphore()

    def one(k, _):
        pl.semaphore_signal(barrier, inc=1, device_id=device(k), device_id_type=MESH)
        return 0

    lax.fori_loop(1, count + 1, one, 0)
    pl.semaphore_wait(barrier, count)


def everyone(at):
    count = at.reps * at.exps

    def device(k):
        other = (at.me + k) % count
        return at.device(other // at.exps, other % at.exps)

    return count - 1, device


def turn(exp, i):
    beside = exp + 1 - 2 * (exp % 2)
    return jnp.where(i == 0, (beside + 2) % 4, jnp.where(i == 1, (exp + 2) % 4, jnp.where(i == 2, beside, exp)))


def lane_of(shape):
    return lax.broadcasted_iota(jnp.int32, shape, 1)


def row_of(shape):
    return lax.broadcasted_iota(jnp.int32, shape, 0)


def bucket_of(offset):
    distance = jnp.abs(offset)
    bucket = jnp.where(offset > 0, 16, 0)
    for threshold in thresholds:
        bucket = bucket + jnp.where(distance >= threshold, 1, 0)
    return bucket


def bits_of(count):
    return count.bit_length() - 1


def column_parts(width):
    tiles = width // 128
    cuts = [0, (tiles + 2) // 3, (2 * tiles + 2) // 3, tiles]
    return [(cuts[i] * 128, (cuts[i + 1] - cuts[i]) * 128) for i in range(3)]


def flipped(place, bit):
    return place + (1 - 2 * ((place // (1 << bit)) % 2)) * (1 << bit)


class Doubling:
    def __init__(self, at, own, every, sems, core_sems, orders):
        self.at, self.own, self.every = at, own, every
        self.sems, self.core_sems, self.orders = sems, core_sems, orders
        self.plane = at.quad * at.exps + at.exp
        self.steps = len(orders[0])
        self.parts = column_parts(own.shape[1])

    def device(self, bit):
        other = flipped(self.plane, bit)
        return (self.at.grp, other // self.at.exps, other % self.at.exps)

    def place(self, part, j):
        p = self.plane
        for i, bit in enumerate(self.orders[part]):
            if (j >> i) & 1:
                p = flipped(p, bit + 1)
        return p

    def block(self, part, p):
        begin, size = self.parts[part]
        return self.every.at[p, :, pl.ds(begin, size)]

    def source(self, part, j):
        begin, size = self.parts[part]
        return self.own.at[:, pl.ds(begin, size)] if j == 0 else self.block(part, self.place(part, j))

    def index(self, step, part, j):
        return part * (1 << self.steps) + (1 << step) - 1 + j

    def copy(self, step, part, j):
        i = self.index(step, part, j)
        return send(
            self.source(part, j),
            self.block(part, self.place(part, j)),
            self.sems.at[0, i],
            self.sems.at[1, i],
            self.device(self.orders[part][step] + 1),
        )

    def core_copy(self, part, j):
        i = part * (1 << self.steps) + j
        return send(
            self.source(part, j),
            self.block(part, self.place(part, j)),
            self.core_sems.at[0, i],
            self.core_sems.at[1, i],
            self.device(0),
        )

    def start(self):
        for part in range(3):
            for step in range(self.steps):
                self.copy(step, part, 0).start()
        for part in range(3):
            self.core_copy(part, 0).start()
        self.keep().start()

    def keep(self):
        return pltpu.make_async_copy(self.own, self.every.at[self.plane], self.core_sems.at[1, 3 << self.steps])

    def next(self, step):
        for part in range(3):
            for j in range(1 << step):
                k = (1 << step) + j
                arrived(self.block(part, self.place(part, k)), self.sems.at[1, self.index(step, part, j)])
                for later in range(step + 1, self.steps):
                    self.copy(later, part, k).start()
                self.core_copy(part, k).start()

    def finish_in(self):
        for part in range(3):
            for j in range(1 << self.steps):
                there = self.block(part, flipped(self.place(part, j), 0))
                arrived(there, self.core_sems.at[1, part * (1 << self.steps) + j])
        self.keep().wait()

    def finish_out(self):
        for part in range(3):
            for j in range(1 << self.steps):
                self.core_copy(part, j).wait_send()
            for step in range(self.steps):
                for j in range(1 << step):
                    self.copy(step, part, j).wait_send()


class Group:
    def __init__(self, at, own, every, sems):
        self.at, self.own, self.every, self.sems = at, own, every, sems
        self.beside, self.across = at.exp + 1 - 2 * (at.exp % 2), (at.exp + 2) % 4

    def copy(self, src, index, send_index, device):
        return send(
            src, self.every.at[index], self.sems.at[0, send_index], self.sems.at[1, index], self.at.device(self.at.rep, device)
        )

    def first(self):
        return [
            self.copy(self.own, self.at.exp, 0, self.across),
            self.copy(self.own, self.at.exp, 1, self.beside),
        ]

    def second(self):
        return self.copy(self.every.at[self.across], self.across, 2, self.beside)

    def start(self):
        for copy in self.first():
            copy.start()

    def pass_on(self):
        arrived(self.every.at[self.across], self.sems.at[1, self.across])
        self.second().start()

    def arrive(self):
        for index in (self.beside, (self.beside + 2) % 4):
            arrived(self.every.at[index], self.sems.at[1, index])

    def sent(self):
        for copy in self.first() + [self.second()]:
            copy.wait_send()


class Tiles:
    def __init__(self, units, reps):
        self.units = units
        self.reps = reps
        self.hidden = units * reps
        self.half = self.hidden // 256
        self.wide = (self.half + 1) // 2
        self.count = 3
        self.size = 128 * self.wide // self.count
        self.skip = 128 * (2 * self.wide - self.half)

    def start(self, quad):
        return 128 * (self.half * (quad // 2) + (self.half - self.wide) * (quad % 2))

    def rows(self, tile):
        result = []
        for k in range(QUAD):
            found = None
            for parity in range(2):
                first = self.start(parity) + tile * self.size
                live = first + (self.skip if parity and tile == 0 else 0)
                begin = max(live, k * self.units)
                end = min(first + self.size, (k + 1) * self.units)
                if end > begin:
                    found = (begin - k * self.units, end - begin, parity, begin - first)
            result.append(found)
        return result


class Outward:
    def __init__(self, at, tiles, tile, in_low, down_slab, both_w, down_w, nothing, sems, down_sems):
        self.at, self.tiles, self.tile = at, tiles, tile
        self.in_low, self.down_slab, self.both_w, self.down_w = in_low, down_slab, both_w, down_w
        self.nothing, self.sems, self.down_sems = nothing, sems, down_sems
        self.slab = in_low.shape[0]

    def source(self, quad, section):
        begin = section * self.tiles.hidden + self.tiles.start(quad) + self.tile * self.tiles.size
        return self.in_low.at[:, pl.ds(pl.multiple_of(begin, 128), self.tiles.size)]

    def target(self, rep, section):
        rows = pl.ds(pl.multiple_of(rep * self.slab, self.slab), self.slab)
        return self.both_w.at[rows, pl.ds(section * self.tiles.size, self.tiles.size)]

    def over(self, act):
        at = self.at

        def one(k, _):
            other = (at.rep + k) % at.reps
            for section in range(2):
                act(
                    functools.partial(
                        send,
                        self.source(other % QUAD, section),
                        self.target(at.rep, section),
                        self.sems.at[0, section * at.reps + other],
                        self.sems.at[1, section * at.reps + at.rep],
                        at.device(other, at.exp),
                    )
                )
            return 0

        lax.fori_loop(1, at.reps, one, 0)

    def over_down(self, act, act_local):
        at = self.at
        for k, piece in enumerate(self.tiles.rows(self.tile)):
            if piece is None:
                continue
            begin, count, parity, to = piece
            quad = 2 * (at.rep // QUAD) + parity
            src, dst = self.down_slab.at[pl.ds(begin, count)], self.down_w.at[pl.ds(to, count)]
            recv = self.down_sems.at[1, at.rep]
            for g in range(at.grps):
                stays = jnp.logical_and(at.grp == g, at.quad == quad)
                ours = at.rep % QUAD == k

                @pl.when(jnp.logical_and(ours, jnp.logical_not(stays)))
                def _():
                    act(functools.partial(send, src, dst, self.down_sems.at[0, g], recv, (g, quad, at.exp)))

                @pl.when(jnp.logical_and(ours, stays))
                def _():
                    act_local(functools.partial(pltpu.make_async_copy, src, dst, recv))

    def blank(self):
        return pltpu.make_async_copy(
            self.nothing, self.down_w.at[pl.ds(0, self.tiles.skip)], self.down_sems.at[1, self.at.reps]
        )

    def start(self):
        at = self.at
        self.over_down(lambda copy: copy().start(), lambda copy: copy().start())
        self.over(lambda copy: copy().start())
        for section in range(2):
            pltpu.make_async_copy(
                self.source(at.quad, section), self.target(at.rep, section), self.sems.at[1, section * at.reps + at.rep]
            ).start()
        if self.tile == 0:

            @pl.when(at.quad % 2 == 1)
            def _():
                self.blank().start()

    def arrive(self):
        at = self.at

        def one(rep, _):
            for section in range(2):
                arrived(self.target(rep, section), self.sems.at[1, section * at.reps + rep])
            return 0

        lax.fori_loop(0, at.reps, one, 0)
        for parity in range(2):

            @pl.when(at.quad % 2 == parity)
            def _():
                for k, piece in enumerate(self.tiles.rows(self.tile)):
                    if piece is not None and piece[2] == parity:
                        source = QUAD * (at.quad // 2) + k
                        arrived(self.down_w.at[pl.ds(piece[3], piece[1])], self.down_sems.at[1, source])
                if parity and self.tile == 0:
                    self.blank().wait()

    def sent(self):
        self.over(lambda copy: copy().wait_send())
        self.over_down(lambda copy: copy().wait_send(), lambda copy: None)


class Homeward:
    def __init__(self, at, tiles, tile, both, down, in_parts, down_parts, sems, down_sems, sections=(0, 1)):
        self.at, self.tiles, self.tile, self.sections = at, tiles, tile, sections
        self.both, self.down, self.in_parts, self.down_parts = both, down, in_parts, down_parts
        self.sems, self.down_sems = sems, down_sems
        self.slab = in_parts.shape[1]

    def target(self, grp, quad, parity, section):
        skip = self.tiles.skip if parity and self.tile == 0 else 0
        to = section * self.tiles.hidden + self.tiles.start(quad) + self.tile * self.tiles.size + skip
        to = to if isinstance(to, int) else pl.multiple_of(to, 128)
        return skip, self.in_parts.at[grp, :, pl.ds(to, self.tiles.size - skip)]

    def copy(self, rep, parity, section, local=False):
        at = self.at
        skip, dst = self.target(at.grp, at.quad, parity, section)
        rows = pl.ds(pl.multiple_of(rep * self.slab, self.slab), self.slab)
        src = self.both.at[rows, pl.ds(section * self.tiles.size + skip, self.tiles.size - skip)]
        recv = self.sems.at[1, section * at.reps + at.rep]
        if local:
            return pltpu.make_async_copy(src, dst, recv)
        return send(src, dst, self.sems.at[0, section * at.reps + rep], recv, at.device(rep, at.exp))

    def over(self, act, act_local):
        at = self.at
        for parity in range(2):

            @pl.when(at.quad % 2 == parity)
            def _():
                def one(k, _):
                    for section in self.sections:
                        act(self.copy((at.rep + k) % at.reps, parity, section))
                    return 0

                lax.fori_loop(1, at.reps, one, 0)
                if act_local:
                    for section in self.sections:
                        act_local(self.copy(at.rep, parity, section, local=True))

    def over_down(self, act, act_local):
        at = self.at
        if self.down is None:
            return
        for k, piece in enumerate(self.tiles.rows(self.tile)):
            if piece is None:
                continue
            begin, count, parity, to = piece
            src, dst = self.down.at[pl.ds(to, count)], self.down_parts.at[at.grp, pl.ds(begin, count)]
            recv = self.down_sems.at[1, at.grp]
            stays = jnp.logical_and(at.grp == at.quad // 2, at.quad == k)
            ours = at.quad % 2 == parity

            @pl.when(jnp.logical_and(ours, jnp.logical_not(stays)))
            def _():
                act(functools.partial(send, src, dst, self.down_sems.at[0, k], recv, (at.quad // 2, k, at.exp)))

            @pl.when(jnp.logical_and(ours, stays))
            def _():
                act_local(functools.partial(pltpu.make_async_copy, src, dst, recv))

    def start(self):
        self.over_down(lambda copy: copy().start(), lambda copy: copy().start())
        self.over(lambda copy: copy.start(), lambda copy: copy.start())

    def arrive(self):
        at = self.at
        for rep in range(at.reps):
            for section in self.sections:
                _, dst = self.target(rep // QUAD, rep % QUAD, rep % 2, section)
                arrived(dst, self.sems.at[1, section * at.reps + rep])
        for k, piece in enumerate(self.tiles.rows(self.tile)):
            if piece is None or self.down is None:
                continue

            @pl.when(at.quad == k)
            def _():
                for g in range(at.grps):
                    arrived(self.down_parts.at[g, pl.ds(piece[0], piece[1])], self.down_sems.at[1, g])

    def sent(self):
        self.over(lambda copy: copy.wait_send(), None)
        self.over_down(lambda copy: copy().wait_send(), lambda copy: None)


def forward_kernel(
    grps,
    exps,
    lengths,
    bias_table,
    routes_t,
    tokens,
    cotangent,
    gains,
    router,
    attn_qkv,
    attn_out,
    expert_in,
    expert_out,
    both_w,
    down_w,
    cot_all,
    n_all,
    comb_all,
    qkv_out,
    lse_out,
    mine_out,
    n1_out,
    wqkv_out,
    wout_out,
    h1_out,
    n2_out,
    probs_out,
    in_out,
    down_out,
    in_wide,
    down_wide,
    qkv_t,
    out_w,
    in_low,
    down_slab,
    tok_all,
    wqkv,
    wout,
    n1,
    qkv,
    lse,
    mine,
    ctx,
    bias,
    comb_send,
    nothing,
    tok_sem,
    wq_sem,
    wo_sem,
    wo2_sem,
    weight_sem,
    down_sem,
    ctx_sem,
    cot_sem,
    cot_core_sem,
    n_sem,
    n_core_sem,
    comb_sem,
    store_sem,
    cast_sem,
):
    at = Where(grps, exps)
    reps = at.reps
    rows, width = tokens.shape
    heads = HEADS // exps
    head_dim = width // HEADS
    head_cols = heads * head_dim
    block_cols = min(128, head_cols)
    shard_cols, row_block = qkv_t.shape
    seg = math.gcd(shard_cols, head_cols)
    segs = shard_cols // seg
    tiles = Tiles(down_slab.shape[0], reps)
    plane = at.quad * exps + at.exp
    members = QUAD * exps
    scale = 1.0 / math.sqrt(head_dim)
    SEND, RECV = 0, 1

    wide_copies = [
        pltpu.make_async_copy(expert_in, in_wide, cast_sem.at[0]),
        pltpu.make_async_copy(expert_out, down_wide, cast_sem.at[1]),
    ]
    for copy in wide_copies:
        copy.start()
    qkv_t[...] = attn_qkv[...].T.astype(low)
    out_w[...] = attn_out[...].astype(low)
    greet(at, *everyone(at))

    def exp_peer(k):
        return (at.exp + k) % exps

    group_tokens = Group(at, tokens, tok_all, tok_sem)
    group_tokens.start()
    tok_all[at.exp] = tokens[...]

    def segment(k):
        col = (at.rep * segs + k) * seg
        section = col // width
        within = col - section * width
        owner = within // head_cols
        return owner, section * head_cols + within - owner * head_cols

    def segment_copy(k, shift):
        owner, offset = segment(k)
        src = qkv_t.at[pl.ds(k * seg, seg)]
        dst = wqkv.at[at.exp, pl.ds(pl.multiple_of(offset, seg), seg)]
        target = at.device((at.rep + shift) % reps, owner)
        return owner, src, dst, functools.partial(
            send, src, dst, wq_sem.at[SEND, k * reps + shift], wq_sem.at[RECV, at.exp * 3 * (head_cols // seg) + offset // seg], target
        )

    def over_segments(act, act_local):
        def one(i, _):
            k, shift = i // reps, i % reps
            owner, src, dst, copy = segment_copy(k, shift)
            stays = jnp.logical_and(shift == 0, owner == at.exp)

            @pl.when(jnp.logical_not(stays))
            def _():
                act(copy())

            @pl.when(stays)
            def _():
                act_local(k, src, dst)

            return 0

        lax.fori_loop(0, segs * reps, one, 0)

    def local_segment(k, src, dst):
        _, offset = segment(k)
        pltpu.make_async_copy(src, dst, wq_sem.at[RECV, at.exp * 3 * (head_cols // seg) + offset // seg]).start()

    over_segments(lambda copy: copy.start(), local_segment)

    for k in range(1, reps):
        other = (at.rep + k) % reps
        send(
            out_w, wout.at[at.exp, at.rep], wo_sem.at[SEND, other], wo_sem.at[RECV, at.rep], at.device(other, at.exp)
        ).start()
    wout[at.exp, at.rep] = out_w[...]
    chip_bits = list(range(bits_of(members) - 1))
    cots = Doubling(at, cotangent, cot_all, cot_sem, cot_core_sem, [chip_bits[::-1]] * 3)
    cots.start()

    span = 2 * rows
    bucket = bucket_of(lane_of((8, span)) - rows)
    for h in range(heads):
        line = jnp.zeros((8, span), full)
        for b in range(BUCKETS):
            line = jnp.where(bucket == b, bias_table[at.exp * heads + h, b], line)
        whole = jnp.broadcast_to(line[0:1], (rows, span))
        bias[h] = pltpu.roll(whole, 0, 1, stride=1, stride_axis=0)[:, rows:]

    group_tokens.pass_on()
    group_tokens.arrive()

    def norm_group(s, _):
        x = tok_all[s].astype(full)
        r = lax.rsqrt(jnp.mean(x * x, axis=1, keepdims=True) + eps_norm)
        n1[s] = (x * r * gains[0:1, :]).astype(low)
        return 0

    lax.fori_loop(0, exps, norm_group, 0)

    for copy in wide_copies:
        copy.wait()
    in_low[...] = in_wide[...].astype(low)
    down_slab[...] = down_wide[...].astype(low)
    nothing[...] = jnp.zeros_like(nothing)
    weights = [
        Outward(
            at, tiles, t, in_low, down_slab, both_w.at[t], down_w.at[t], nothing, weight_sem.at[t], down_sem.at[t]
        )
        for t in range(2)
    ]
    weights[0].start()

    def wait_segment(i, _):
        e, j = i // (3 * head_cols // seg), i % (3 * head_cols // seg)
        arrived(wqkv.at[e, pl.ds(pl.multiple_of(j * seg, seg), seg)], wq_sem.at[RECV, i])
        return 0

    lax.fori_loop(0, exps * 3 * head_cols // seg, wait_segment, 0)

    def project(s, _):
        total = jnp.zeros((rows, 3 * head_cols), full)
        for e in range(exps):
            total = total + nt(n1[s, :, e * row_block : (e + 1) * row_block], wqkv[e])
        qkv[s] = total.astype(low)
        return 0

    lax.fori_loop(0, exps, project, 0)

    group_wout = Group(at, wout.at[at.exp], wout, wo2_sem)

    def beside(k):
        if k == 1:
            for j in range(1, reps):
                other = (at.rep + j) % reps
                arrived(wout.at[at.exp, other], wo_sem.at[RECV, other])
            group_wout.start()
        elif k == 2:
            cots.next(0)
        else:
            group_wout.pass_on()

    def attend(i, _):
        s = turn(at.exp, i)
        for k in range(1, exps):

            @pl.when(i == k)
            def _():
                beside(k)

        ok = lane_of((rows, rows)) < lengths[at.base + s]
        lane = lane_of((rows, block_cols))
        sums = jnp.zeros((rows, 128), full)
        for c in range(head_cols // block_cols):
            cols = slice(c * block_cols, (c + 1) * block_cols)
            q = qkv[s, :, cols] * scale
            k = qkv[s, :, head_cols + c * block_cols : head_cols + (c + 1) * block_cols]
            v = qkv[s, :, 2 * head_cols + c * block_cols : 2 * head_cols + (c + 1) * block_cols]
            result = jnp.zeros((rows, block_cols), full)
            for t in range(block_cols // head_dim):
                h = c * (block_cols // head_dim) + t
                here = jnp.logical_and(lane >= t * head_dim, lane < (t + 1) * head_dim)
                scores = nt(jnp.where(here, q, jnp.zeros_like(q)), k) + bias[h]
                scores = jnp.where(ok, scores, -1e30)
                top = jnp.max(scores, axis=1, keepdims=True)
                weights = jnp.exp(scores - top)
                total = jnp.sum(weights, axis=1, keepdims=True)
                weights = (weights * (1.0 / total)).astype(low)
                result = jnp.where(here, jnp.dot(weights, v, preferred_element_type=full), result)
                sums = jnp.where(lane_of((rows, 128)) == h, top + jnp.log(total), sums)
            mine[s, :, cols] = result.astype(low)
        lse[s] = sums

        @pl.when(i < exps - 1)
        def _():
            send(
                mine.at[s], ctx.at[at.exp], ctx_sem.at[SEND, s], ctx_sem.at[RECV, at.exp], at.device(at.rep, s)
            ).start()

        @pl.when(i == exps - 1)
        def _():
            pltpu.make_async_copy(mine.at[s], ctx.at[at.exp], ctx_sem.at[RECV, at.exp]).start()

        return 0

    lax.fori_loop(0, exps, attend, 0)

    cots.next(1)
    group_wout.arrive()
    for e in range(exps):
        arrived(ctx.at[e], ctx_sem.at[RECV, e])

    out_cols = wout.shape[3]
    for r in range(reps):
        cols = slice(r * out_cols, (r + 1) * out_cols)
        total = tokens[:, cols].astype(full)
        for e in range(exps):
            total = total + jnp.dot(ctx[e], wout[e, r], preferred_element_type=full)
        h1_out[:, cols] = total
    h1 = h1_out[...]
    r2 = lax.rsqrt(jnp.mean(h1 * h1, axis=1, keepdims=True) + eps_norm)
    n2 = (h1 * r2 * gains[1:2, :]).astype(low)
    n2_out[...] = n2
    rotated = [chip_bits[c:] + chip_bits[:c] for c in range(3)]
    rows_two = Doubling(at, n2_out, n_all, n_sem, n_core_sem, rotated)
    rows_two.start()
    weights[1].start()

    router_rows = jnp.concatenate([router[...], jnp.zeros((128 - exps, width), full)], axis=0)
    logits = nt(n2.astype(full), router_rows, precision=highest)
    lane = lane_of((rows, 128))
    logits = jnp.where(lane < exps, logits, -1e30)
    probs = jnp.exp(logits - jnp.max(logits, axis=1, keepdims=True))
    probs = probs / jnp.sum(probs, axis=1, keepdims=True)
    probs_out[...] = probs
    picked = jnp.where(routed(routes_t, at.me, rows), probs, 0.0)
    comb = picked / jnp.sum(picked, axis=1, keepdims=True)
    comb = jnp.where(row_of((rows, 1)) < lengths[at.me], comb, 0.0)
    comb_send[...] = comb.T[0 : comb_send.shape[0]]

    def comb_copy(k):
        other = (plane + k) % members
        return send(
            comb_send,
            comb_all.at[plane],
            comb_sem.at[SEND, other],
            comb_sem.at[RECV, plane],
            (at.grp, other // exps, other % exps),
        )

    def start_comb(k, _):
        comb_copy(k).start()
        return 0

    lax.fori_loop(1, members, start_comb, 0)
    pltpu.make_async_copy(comb_send, comb_all.at[plane], comb_sem.at[RECV, plane]).start()
    rows_two.next(0)

    stores = [
        (qkv, qkv_out),
        (lse, lse_out),
        (mine, mine_out),
        (n1, n1_out),
        (wqkv, wqkv_out),
        (wout, wout_out),
        (in_low, in_out),
        (down_slab, down_out),
    ]
    for i, (src, dst) in enumerate(stores):
        pltpu.make_async_copy(src, dst, store_sem.at[i]).start()

    for step in range(1, rows_two.steps):
        rows_two.next(step)
    for step in range(2, cots.steps):
        cots.next(step)

    cots.finish_in()
    rows_two.finish_in()

    def comb_in(k, _):
        arrived(comb_all.at[k], comb_sem.at[RECV, k])
        return 0

    lax.fori_loop(0, members, comb_in, 0)
    for tile in weights:
        tile.arrive()

    for k in range(1, exps):
        peer = exp_peer(k)
        arrived(mine.at[peer], ctx_sem.at[SEND, peer])
    over_segments(lambda copy: copy.wait_send(), lambda k, src, dst: None)
    for k in range(1, reps):
        arrived(out_w, wo_sem.at[SEND, (at.rep + k) % reps])
    group_tokens.sent()
    group_wout.sent()
    cots.finish_out()
    rows_two.finish_out()

    def sent_comb(k, _):
        comb_copy(k).wait_send()
        return 0

    lax.fori_loop(1, members, sent_comb, 0)
    for tile in weights:
        tile.sent()
    for i, (src, dst) in enumerate(stores):
        pltpu.make_async_copy(src, dst, store_sem.at[i]).wait()


def forward_call(
    grps, exps, lengths, bias_table, routes_t, tokens, cotangent, gains, router, attn_qkv, attn_out, expert_in, expert_out
):
    reps = grps * QUAD
    rows, width = tokens.shape
    head_cols = width // exps
    row_block, shard_cols = attn_qkv.shape
    seg = math.gcd(shard_cols, head_cols)
    segs = shard_cols // seg
    units = expert_out.shape[0]
    out_cols = attn_out.shape[1]
    heads = HEADS // exps
    members = QUAD * exps
    tiles = Tiles(units, reps)
    shape = jax.ShapeDtypeStruct
    vmem = pl.BlockSpec(memory_space=pltpu.VMEM)
    smem = pl.BlockSpec(memory_space=pltpu.SMEM)
    hbm = pl.BlockSpec(memory_space=pl.ANY)
    results = [
        (shape((2, width, 2 * tiles.size), low), hbm),
        (shape((2, tiles.size, width), low), hbm),
        (shape((members, rows, width), low), hbm),
        (shape((members, rows, width), low), hbm),
        (shape((members, 8, rows), full), hbm),
        (shape((exps, rows, 3 * head_cols), low), hbm),
        (shape((exps, rows, 128), full), hbm),
        (shape((exps, rows, head_cols), low), hbm),
        (shape((exps, rows, width), low), hbm),
        (shape((exps, 3 * head_cols, row_block), low), hbm),
        (shape((exps, reps, row_block, out_cols), low), hbm),
        (shape((rows, width), full), vmem),
        (shape((rows, width), low), vmem),
        (shape((rows, 128), full), vmem),
        (shape(expert_in.shape, low), hbm),
        (shape(expert_out.shape, low), hbm),
    ]
    dma = pltpu.SemaphoreType.DMA
    chips = members // 2
    return pl.pallas_call(
        functools.partial(forward_kernel, grps, exps),
        out_shape=[r[0] for r in results],
        in_specs=[smem] * 2 + [vmem] * 7 + [hbm] * 2,
        out_specs=[r[1] for r in results],
        scratch_shapes=[
            pltpu.VMEM(expert_in.shape, full),
            pltpu.VMEM(expert_out.shape, full),
            pltpu.VMEM((shard_cols, row_block), low),
            pltpu.VMEM((row_block, out_cols), low),
            pltpu.VMEM(expert_in.shape, low),
            pltpu.VMEM(expert_out.shape, low),
            pltpu.VMEM((exps, rows, width), low),
            pltpu.VMEM((exps, 3 * head_cols, row_block), low),
            pltpu.VMEM((exps, reps, row_block, out_cols), low),
            pltpu.VMEM((exps, rows, width), low),
            pltpu.VMEM((exps, rows, 3 * head_cols), low),
            pltpu.VMEM((exps, rows, 128), full),
            pltpu.VMEM((exps, rows, head_cols), low),
            pltpu.VMEM((exps, rows, head_cols), low),
            pltpu.VMEM((heads, rows, rows), full),
            pltpu.VMEM((8, rows), full),
            pltpu.VMEM((tiles.skip, width), low),
            dma((2, exps)),
            dma((2, max(segs * reps, exps * 3 * head_cols // seg))),
            dma((2, reps)),
            dma((2, exps)),
            dma((2, 2, 2 * reps)),
            dma((2, 2, reps + 1)),
            dma((2, exps)),
            dma((2, 3 * chips)),
            dma((2, 3 * chips + 1)),
            dma((2, 3 * chips)),
            dma((2, 3 * chips + 1)),
            dma((2, members)),
            dma((8,)),
            dma((2,)),
        ],
        compiler_params=pltpu.CompilerParams(
            collective_id=0, has_side_effects=True, vmem_limit_bytes=60 * 1024 * 1024
        ),
        name="forward",
    )(lengths, bias_table, routes_t, tokens, cotangent, gains, router, attn_qkv, attn_out, expert_in, expert_out)


def expert_kernel(
    grps,
    exps,
    cap,
    deal,
    routes_t,
    comb,
    n_all,
    cot_all,
    both_w,
    down_w,
    in_low,
    down_slab,
    h1,
    n_half,
    y_half,
    n_far,
    y_far,
    c_sum,
    both_g,
    down_g,
    in_parts,
    down_parts,
    place,
    marks,
    n_rows,
    g_rows,
    both_v,
    down_v,
    raw_n,
    raw_g,
    y_acc,
    n_acc,
    both_d,
    active,
    both_stage,
    down_stage,
    out_n,
    out_y,
    load_sem,
    raw_sem,
    out_sem,
    in_sem,
    in_down_sem,
    home_sem,
    home_down_sem,
    stage_sem,
    far_sem,
):
    at = Where(grps, exps)
    rows, width = n_all.shape[1:]
    tiles = Tiles(down_slab.shape[0], at.reps)
    size = tiles.size
    slots = exps * cap
    members = QUAD * exps
    loads = [pltpu.make_async_copy(both_w.at[t], both_v.at[t], load_sem.at[0, t]) for t in range(2)] + [
        pltpu.make_async_copy(down_w.at[t], down_v.at[t], load_sem.at[1, t]) for t in range(2)
    ]
    for copy in loads:
        copy.start()

    def raw_copies(q):
        here = pl.ds(pl.multiple_of(q * exps, exps), exps)
        return [
            pltpu.make_async_copy(n_all.at[here], raw_n.at[q % 2], raw_sem.at[0, q % 2]),
            pltpu.make_async_copy(cot_all.at[here], raw_g.at[q % 2], raw_sem.at[1, q % 2]),
        ]

    for copy in raw_copies(0):
        copy.start()

    def partner(k):
        rep = jnp.where(k < at.reps, (at.rep + k) % at.reps, at.rep)
        return at.device(rep, jnp.where(k < at.reps, at.exp, beside))

    beside = at.exp + 1 - 2 * (at.exp % 2)
    greet(at, at.reps, partner)
    last = tiles.count - 1
    incoming = Outward(
        at, tiles, last, in_low, down_slab, both_v.at[last], down_v.at[last], None, in_sem, in_down_sem
    )
    incoming.start()
    home = Homeward(
        at, tiles, 0, both_stage.at[0], down_stage.at[0], in_parts, down_parts, home_sem, home_down_sem, (0,)
    )

    earlier = jnp.where(row_of((rows, rows)) < lane_of((rows, rows)), 1.0, 0.0).astype(low)
    slot = row_of((cap, rows)).astype(full)

    def dispatch(q, _):
        @pl.when(q + 1 < QUAD)
        def _():
            for copy in raw_copies(q + 1):
                copy.start()

        for copy in raw_copies(q):
            copy.wait()
        lines = []
        for j in range(exps):
            seq = at.grp * members + q * exps + j
            pair = routes_t[:, pl.ds(pl.multiple_of(seq * rows, rows), rows)]
            lines.append(jnp.logical_or(pair[0:1] == at.exp, pair[1:2] == at.exp))
        lines = [jnp.where(line, 1.0, 0.0) for line in lines] + [jnp.zeros((8 - exps, rows), full)]
        hot_low = jnp.concatenate(lines, axis=0).astype(low)
        before = dot(hot_low, earlier)
        for j in range(exps):
            s = q * exps + j
            inside = jnp.logical_and(slot == before[j : j + 1, :], hot_low[j : j + 1, :].astype(full) > 0.5)
            here = jnp.where(inside, 1.0, 0.0)
            place[s] = here.astype(low)
            g = raw_g[q % 2, 0]
            for b in range(1, exps):
                g = jnp.where(deal[at.grp * members + s] == at.grp * members + q * exps + b, raw_g[q % 2, b], g)
            where = pl.ds(pl.multiple_of(s * cap, cap), cap)
            n_rows[where] = dot(here.astype(low), raw_n[q % 2, j]).astype(low)
            g_rows[where] = dot(here.astype(low), g).astype(low)
            marks[where, 0:1] = jnp.sum(here * comb[s, pl.ds(at.exp, 1), :], axis=1, keepdims=True)
            marks[where, 1:2] = jnp.zeros((cap, 1), full)
        return 0

    lax.fori_loop(0, QUAD, dispatch, 0)
    for copy in loads:
        copy.wait()
    curve = math.sqrt(2.0 / math.pi)

    core = at.exp % 2

    def half_copies(j):
        return [
            pltpu.make_async_copy(out_n.at[j % 2], n_half.at[j], out_sem.at[0, j % 2]),
            pltpu.make_async_copy(out_y.at[j % 2], y_half.at[j], out_sem.at[1, j % 2]),
        ]

    def far_copies(j):
        device = at.device(at.rep, beside)
        return [
            send(raw.at[j // exps, j % exps], far.at[j], far_sem.at[i, 0, j], far_sem.at[i, 1, j], device)
            for i, (raw, far) in enumerate(((raw_n, n_far), (raw_g, y_far)))
        ]

    def slots_of(s):
        return pl.ds(pl.multiple_of(s * cap, cap), cap)

    def n_rows_of(s):
        where = slots_of(s)
        line = jnp.sum(place[s].astype(full) * marks[where, 1:2], axis=0, keepdims=True)
        c_sum[s] = jnp.broadcast_to(line, (8, rows))
        return tn(place[s], n_acc[where].astype(low)).astype(low)

    def y_rows_of(p):
        first = p // exps * exps
        spot = at.grp * members + p
        here, y = place[first], y_acc[slots_of(first)]
        for c in range(1, exps):
            taken = deal[at.grp * members + first + c] == spot
            here = jnp.where(taken, place[first + c], here)
            y = jnp.where(taken, y_acc[slots_of(first + c)], y)
        return (tn(here, y) + jnp.where(deal[at.me] == spot, h1[...], 0.0)).astype(low)

    def give_back(j, _):
        @pl.when(j >= 2)
        def _():
            for copy in half_copies(j - 2):
                copy.wait()

        out_n[j % 2] = n_rows_of(2 * j + core)
        out_y[j % 2] = y_rows_of(2 * j + core)
        for copy in half_copies(j):
            copy.start()
        raw_n[j // exps, j % exps] = n_rows_of(2 * j + 1 - core)
        raw_g[j // exps, j % exps] = y_rows_of(2 * j + 1 - core)
        for copy in far_copies(j):
            copy.start()
        return 0

    def tile_work(f, _):
        @pl.when(f == last)
        def _():
            incoming.arrive()

        def chunk(c, _):
            here = pl.ds(pl.multiple_of(c * slots, slots), slots)
            share = marks[here, 0:1]
            both = dot(n_rows[here], both_v[f])
            gate_part, up_part = both[:, :size], both[:, size:]
            grad = nt(g_rows[here], down_v[f])
            square = gate_part * gate_part
            bend = jnp.tanh(curve * gate_part * (1.0 + 0.044715 * square))
            half = 0.5 * (1.0 + bend)
            gelu = gate_part * half
            slope = half + (0.5 * curve) * gate_part * (1.0 - bend * bend) * (1.0 + (3 * 0.044715) * square)
            value = gelu * up_part
            marks[here, 1:2] += jnp.sum(value * grad, axis=1, keepdims=True)
            grad = grad * share
            active[here] = (value * share).astype(low)
            both_d[here, :size] = (grad * up_part * slope).astype(low)
            both_d[here, size:] = (grad * gelu).astype(low)
            y = dot(active[here], down_v[f])
            y_acc[here] = jnp.where(f == 0, y, y_acc[here].astype(full) + y).astype(low)
            n_back = nt(both_d[here], both_v[f])
            n_acc[here] = jnp.where(f == 0, n_back, n_acc[here] + n_back)
            return 0

        lax.fori_loop(0, QUAD, chunk, 0)

        @pl.when(f == last)
        def _():
            lax.fori_loop(0, members // 2, give_back, 0)

        def columns(m, _):
            cols = pl.ds(pl.multiple_of(m * (width // 2), width // 2), width // 2)
            both_stage[f, cols] = tn(n_rows[:, cols], both_d[...]).astype(low)
            down_stage[f, :, cols] = tn(active[...], g_rows[:, cols]).astype(low)
            return 0

        lax.fori_loop(0, 2, columns, 0)

        for copy in stage_copies(f):
            copy.start()

        @pl.when(f == 0)
        def _():
            home.start()

        @pl.when(f > 0)
        def _():
            down_copy(f).start()

        return 0

    def stage_copies(f):
        return [pltpu.make_async_copy(both_stage.at[f], both_g.at[f], stage_sem.at[0, f])]

    def down_copy(f):
        return pltpu.make_async_copy(down_stage.at[f], down_g.at[f - 1], stage_sem.at[1, f])

    lax.fori_loop(0, tiles.count, tile_work, 0)

    for j in (members // 2 - 2, members // 2 - 1):
        for copy in half_copies(j):
            copy.wait()
    for f in range(tiles.count):
        for copy in stage_copies(f):
            copy.wait()
        if f:
            down_copy(f).wait()

    def core_in(j, _):
        for copy in far_copies(j):
            copy.wait_send()
        arrived(n_far.at[j], far_sem.at[0, 1, j])
        arrived(y_far.at[j], far_sem.at[1, 1, j])
        return 0

    lax.fori_loop(0, members // 2, core_in, 0)
    home.arrive()
    incoming.sent()
    home.sent()


def expert_call(grps, exps, cap, deal, routes_t, comb_all, n_all, cot_all, both_w, down_w, in_low, down_slab, h1):
    members, rows, width = n_all.shape
    reps = grps * QUAD
    tiles = Tiles(down_slab.shape[0], reps)
    size = tiles.size
    slab, both_hidden = in_low.shape
    units = down_slab.shape[0]
    slots = exps * cap
    shape = jax.ShapeDtypeStruct
    vmem = pl.BlockSpec(memory_space=pltpu.VMEM)
    smem = pl.BlockSpec(memory_space=pltpu.SMEM)
    hbm = pl.BlockSpec(memory_space=pl.ANY)
    results = [
        (shape((members // 2, rows, width), low), hbm),
        (shape((members // 2, rows, width), low), hbm),
        (shape((members // 2, rows, width), low), hbm),
        (shape((members // 2, rows, width), low), hbm),
        (shape((members, 8, rows), full), vmem),
        (shape((tiles.count, width, 2 * size), low), hbm),
        (shape((2, size, width), low), hbm),
        (shape((grps, slab, both_hidden), low), hbm),
        (shape((grps, units, width), low), hbm),
    ]
    dma = pltpu.SemaphoreType.DMA
    return pl.pallas_call(
        functools.partial(expert_kernel, grps, exps, cap),
        out_shape=[r[0] for r in results],
        in_specs=[smem] + [vmem] * 2 + [hbm] * 6 + [vmem],
        out_specs=[r[1] for r in results],
        scratch_shapes=[
            pltpu.VMEM((members, cap, rows), low),
            pltpu.VMEM((QUAD * slots, 128), full),
            pltpu.VMEM((QUAD * slots, width), low),
            pltpu.VMEM((QUAD * slots, width), low),
            pltpu.VMEM((tiles.count, width, 2 * size), low),
            pltpu.VMEM((tiles.count, size, width), low),
            pltpu.VMEM((2, exps, rows, width), low),
            pltpu.VMEM((2, exps, rows, width), low),
            pltpu.VMEM((QUAD * slots, width), low),
            pltpu.VMEM((QUAD * slots, width), full),
            pltpu.VMEM((QUAD * slots, 2 * size), low),
            pltpu.VMEM((QUAD * slots, size), low),
            pltpu.VMEM((tiles.count, width, 2 * size), low),
            pltpu.VMEM((tiles.count, size, width), low),
            pltpu.VMEM((2, rows, width), low),
            pltpu.VMEM((2, rows, width), low),
            dma((2, 2)),
            dma((2, 2)),
            dma((2, 2)),
            dma((2, 2 * reps)),
            dma((2, reps + 1)),
            dma((2, 2 * reps)),
            dma((2, max(QUAD, grps))),
            dma((2, tiles.count)),
            dma((2, 2, members // 2)),
        ],
        compiler_params=pltpu.CompilerParams(
            collective_id=2, has_side_effects=True, vmem_limit_bytes=60 * 1024 * 1024
        ),
        name="experts",
    )(deal, routes_t, comb_all, n_all, cot_all, both_w, down_w, in_low, down_slab, h1)


def adam_kernel(exps, *refs):
    in_parts, down_parts, qkv_grad, out_grad, small = refs[:5]
    states, news, bias_grad = refs[5:26], refs[26:47], refs[47]
    heads = HEADS // exps
    width = small.shape[1]

    def update(i, grad, rate, decay):
        weight, first, second = [state[...] for state in states[3 * i : 3 * i + 3]]
        values = adamw_update(weight, first, second, grad, rate, decay)
        for new, value in zip(news[3 * i : 3 * i + 3], values, strict=True):
            new[...] = value

    def total(parts):
        result = parts[0].astype(full)
        for k in range(1, parts.shape[0]):
            result = result + parts[k].astype(full)
        return result

    @pl.when(pl.program_id(0) == 0)
    def _():
        update(0, qkv_grad[...], 1.5 / math.sqrt(D), 0.1)
        update(1, out_grad[...], 6.0 / math.sqrt(D), 0.1)
        for e in range(exps):
            for h in range(heads):
                bias_grad[e * heads + h : e * heads + h + 1, :] = small[
                    exps + 3 + e : exps + 4 + e, h * 128 : h * 128 + BUCKETS
                ]
        update(2, bias_grad[...], 0.3, 0.0)
        update(3, small[0:exps, :], 1.0 / math.sqrt(D), 0.1)
        update(4, small[exps : exps + 2, :], 0.5, 0.0)

    update(5, total(in_parts), 1.5 / math.sqrt(D), 0.1)
    update(6, total(down_parts), 1.5 / math.sqrt(FF), 0.1)


def adam_call(exps, in_parts, down_parts, qkv_grad, out_grad, small, states):
    steps = 11

    def whole(array):
        return pl.BlockSpec(array.shape, lambda i: (0,) * array.ndim)

    def columns(array):
        block = array.shape[:-1] + (array.shape[-1] // steps,)
        return pl.BlockSpec(block, lambda i: (0,) * (array.ndim - 1) + (i,))

    def lines(array):
        lead = array.shape[:-2]
        block = lead + (array.shape[-2] // steps, array.shape[-1])
        return pl.BlockSpec(block, lambda i: (0,) * len(lead) + (i, 0))

    specs = [whole(state) for state in states[:15]]
    specs += [columns(state) for state in states[15:18]] + [lines(state) for state in states[18:]]
    return pl.pallas_call(
        functools.partial(adam_kernel, exps),
        grid=(steps,),
        in_specs=[columns(in_parts), lines(down_parts), whole(qkv_grad), whole(out_grad), whole(small)] + specs,
        out_specs=specs,
        out_shape=[jax.ShapeDtypeStruct(state.shape, full) for state in states],
        scratch_shapes=[pltpu.VMEM((HEADS, BUCKETS), full)],
        compiler_params=pltpu.CompilerParams(vmem_limit_bytes=60 * 1024 * 1024),
        name="adam",
    )(in_parts, down_parts, qkv_grad, out_grad, small, *states)


class Halving:
    def __init__(self, at, half, far, kept, bufs, sems, load_sem, orders):
        self.at, self.half, self.far, self.kept, self.bufs = at, half, far, kept, bufs
        self.sems, self.load_sem = sems, load_sem
        self.plane = at.quad * at.exps + at.exp
        self.places = bits_of(QUAD * at.exps)
        self.chip_bits = list(range(self.places - 1))
        self.parts = column_parts(half.shape[2])
        self.orders = orders

    def device(self, bit):
        other = flipped(self.plane, bit)
        return (self.at.grp, other // self.at.exps, other % self.at.exps)

    def loads(self, j):
        return [
            pltpu.make_async_copy(self.far.at[j], self.bufs[0].at[j], self.load_sem.at[0, j]),
            pltpu.make_async_copy(self.half.at[j], self.kept.at[j], self.load_sem.at[1, j]),
        ]

    def start_first(self):
        def one(j, _):
            for copy in self.loads(j):
                copy.start()
            return 0

        lax.fori_loop(0, self.half.shape[0], one, 0)

    def add_first(self):
        def one(j, _):
            for copy in self.loads(j):
                copy.wait()
            self.bufs[0][j] = self.bufs[0][j] + self.kept[j]
            return 0

        lax.fori_loop(0, self.half.shape[0], one, 0)

    def hop(self, step, part):
        order = self.orders[part]
        bit = order[step]
        left = [b for b in self.chip_bits if b not in order[:step]]
        pos = left.index(bit)
        half = 1 << (len(left) - 1)
        mine = (self.plane // (1 << (bit + 1))) % 2
        device = self.device(bit + 1)
        begin, size = self.parts[part]
        cols = pl.ds(begin, size)
        base = self.base(step, part)

        def index(j, value):
            return (j >> pos) * (1 << (pos + 1)) + value * (1 << pos) + j % (1 << pos)

        pairs = []
        for j in range(half):
            copy = functools.partial(
                send,
                self.bufs[step].at[index(j, 1 - mine), :, cols],
                self.bufs[step + 1].at[j, :, cols],
                self.sems.at[0, base + j],
                self.sems.at[1, base + j],
                device,
            )
            pairs.append((copy, index(j, mine), j))
        return pairs, begin, size, base

    def base(self, step, part):
        n = len(self.chip_bits)
        return part * (1 << n) + sum(1 << (n - 1 - s) for s in range(step))

    def start(self, step, part=None):
        for p in range(3) if part is None else [part]:
            for copy, _, _ in self.hop(step, p)[0]:
                copy().start()

    def add(self, step, part):
        pairs, begin, size, base = self.hop(step, part)
        cols = pl.ds(begin, size)
        here, there = self.bufs[step], self.bufs[step + 1]
        for _, keep, j in pairs:
            arrived(there.at[j, :, cols], self.sems.at[1, base + j])
            there[j, :, begin : begin + size] = (
                there[j, :, begin : begin + size] + here[keep, :, begin : begin + size]
            )

    def next(self, step):
        for p in range(3):
            self.add(step, p)
            if step + 1 < len(self.chip_bits):
                self.start(step + 1, p)

    def result(self):
        return self.bufs[len(self.chip_bits)]

    def finish(self):
        for step in range(len(self.chip_bits)):
            for p in range(3):
                for copy, _, _ in self.hop(step, p)[0]:
                    copy().wait_send()


def backward_kernel(
    grps,
    exps,
    lengths,
    deal,
    bias_table,
    n_half,
    y_half,
    n_far,
    y_far,
    c_parts,
    both_g,
    down_g,
    in_before,
    down_before,
    n1_in,
    cot_all,
    routes_t,
    tokens,
    n2_in,
    probs_in,
    h1_from,
    qkv_from,
    lse_from,
    mine_from,
    wqkv_from,
    wout_from,
    gains,
    router_t,
    *rest,
):
    token_grad, block_out, in_parts, down_parts, qkv_grad, out_grad, small_out = rest[:7]
    scratch = rest[7:]
    (
    h1_in,
    qkv,
    lse,
    mine,
    wqkv,
    wout,
    kept,
    n_bufs,
    y_bufs,
    c_in,
    dh1,
    dz_send,
    dz_all,
    do_send,
    do_in,
    bias,
    bias_sum,
    dqkv,
    dqkv_t,
    dn1_send,
    dn1_in,
    wq_send,
    og_send,
    mids,
    far_send,
    far_in,
    small_send,
    small_exp,
    small_sum,
    small_rep,
    n_sem,
    y_sem,
    load_sem,
    c_sem,
    weight_sem,
    down_sem,
    dz_sem,
    do_sem,
    dn1_sem,
    wq_sem,
    og_sem,
    mid_sem,
    far_sem,
    small_sem,
    small2_sem,
    n1_sem,
    operand_sem,
    ) = scratch
    at = Where(grps, exps)
    reps = at.reps
    rows, width = tokens.shape
    heads = HEADS // exps
    head_dim = width // HEADS
    head_cols = heads * head_dim
    block_cols = min(128, head_cols)
    row_block = wqkv.shape[2]
    out_cols = wout.shape[3]
    tiles = Tiles(down_parts.shape[1], reps)
    scale = 1.0 / math.sqrt(head_dim)
    SEND, RECV = 0, 1
    plane = at.quad * exps + at.exp
    members = QUAD * exps

    def exp_peer(k):
        return (at.exp + k) % exps

    router = router_t[...]
    n1 = kept.at[0:exps]
    group = pl.ds(pl.multiple_of(at.quad * exps, exps), exps)
    cot_copy = pltpu.make_async_copy(cot_all.at[group], dn1_send, n1_sem.at[1])
    cot_copy.start()
    loads = [
        pltpu.make_async_copy(src, dst, operand_sem.at[i])
        for i, (src, dst) in enumerate(
            ((h1_from, h1_in), (wout_from, wout), (qkv_from, qkv), (lse_from, lse), (mine_from, mine), (wqkv_from, wqkv))
        )
    ]
    dn = Halving(at, n_half, n_far, kept, n_bufs, n_sem, load_sem.at[0], [[0, 1, 2], [1, 2, 0], [2, 0, 1]])
    ys = Halving(at, y_half, y_far, kept, y_bufs, y_sem, load_sem.at[1], [[1, 0, 2], [1, 0, 2], [0, 1, 2]])
    dn.start_first()
    for copy in loads:
        copy.start()

    def partner(k):
        other = (plane + k) % members
        rest = k - members
        grp = jnp.where(k < members, at.grp, (at.grp + 1 + rest // QUAD) % grps)
        quad = jnp.where(k < members, other // exps, rest % QUAD)
        return grp, quad, jnp.where(k < members, other % exps, at.exp)

    greet(at, members - 1 + QUAD * (grps - 1), partner)

    homes = [
        Homeward(
            at,
            tiles,
            t,
            both_g.at[t],
            down_g.at[t - 1] if t else None,
            in_parts,
            down_parts,
            weight_sem.at[t],
            down_sem.at[t],
            (0, 1) if t else (1,),
        )
        for t in range(tiles.count)
    ]
    dn.add_first()
    dn.start(0)
    ys.start_first()
    homes[0].start()
    n1_copy = pltpu.make_async_copy(n1_in, n1, n1_sem.at[0])

    def c_copy(k):
        other = (plane + k) % members
        return other, send(
            c_parts.at[other],
            c_in.at[plane],
            c_sem.at[SEND, other],
            c_sem.at[RECV, plane],
            (at.grp, other // exps, other % exps),
        )

    def start_c(k, _):
        c_copy(k)[1].start()
        return 0

    lax.fori_loop(1, members, start_c, 0)
    pltpu.make_async_copy(c_parts.at[plane], c_in.at[plane], c_sem.at[RECV, plane]).start()

    span = 2 * rows
    bucket = bucket_of(lane_of((8, span)) - rows)
    for h in range(heads):
        line = jnp.zeros((8, span), full)
        for b in range(BUCKETS):
            line = jnp.where(bucket == b, bias_table[at.exp * heads + h, b], line)
        whole = jnp.broadcast_to(line[0:1], (rows, span))
        bias[h] = pltpu.roll(whole, 0, 1, stride=1, stride_axis=0)[:, rows:]


    def wait_c(k, _):
        arrived(c_in.at[k], c_sem.at[RECV, k])
        return 0

    lax.fori_loop(0, members, wait_c, 0)
    lane = lane_of((rows, 128))
    comb_rows = []
    for e in range(exps):
        total = c_in[e]
        for q in range(1, QUAD):
            total = total + c_in[q * exps + e]
        comb_rows.append(total[0:1, :])
    comb_rows.append(jnp.zeros((128 - exps, rows), full))
    comb_grad = jnp.concatenate(comb_rows, axis=0).T
    valid = row_of((rows, 1)) < lengths[at.me]
    probs = probs_in[...]
    hot = routed(routes_t, at.me, rows)
    picked = jnp.where(hot, probs, 0.0)
    total = jnp.sum(picked, axis=1, keepdims=True)
    gate = picked / total
    gate_grad_rows = jnp.where(valid, comb_grad, 0.0)
    spread_grad = jnp.sum(gate_grad_rows * gate, axis=1, keepdims=True)
    probs_grad = jnp.where(hot, (gate_grad_rows - spread_grad) / total, 0.0)
    logit_grad = probs * (probs_grad - jnp.sum(probs_grad * probs, axis=1, keepdims=True))
    n2 = n2_in[...].astype(full)
    router_rows = lax.dot_general(
        logit_grad, n2, (((0,), (0,)), ((), ())), preferred_element_type=full, precision=highest
    )
    small_rows = small_send.shape[0]
    small_send[...] = jnp.zeros_like(small_send)
    small_send[0:exps, :] = router_rows[0:exps, :]
    router_back = jnp.dot(
        logit_grad, jnp.concatenate([router, jnp.zeros((128 - exps, width), full)], axis=0),
        precision=highest, preferred_element_type=full,
    )
    for copy in loads:
        copy.wait()
    h1 = h1_in[...]
    r2 = lax.rsqrt(jnp.mean(h1 * h1, axis=1, keepdims=True) + eps_norm)

    dn.next(0)
    ys.add_first()
    n1_copy.start()
    dn.next(1)
    homes[1].start()
    steps = len(dn.chip_bits)
    for step in range(2, steps):
        dn.next(step)

    n2_grad = router_back + dn.result()[0].astype(full)
    scaled = n2_grad * gains[1:2, :]
    cot_copy.wait()
    dealt = deal[at.me] - at.base
    g = dn1_send[0]
    for e in range(1, exps):
        g = jnp.where(dealt == e, dn1_send[e], g)
    hidden_grad = (
        jnp.where(valid, g.astype(full), 0.0)
        + r2 * scaled
        - h1 * (r2 * r2 * r2) * jnp.mean(scaled * h1, axis=1, keepdims=True)
    )
    dh1[...] = hidden_grad
    small_send[exps + 1 : exps + 2, :] = jnp.sum(n2_grad * h1 * r2, axis=0, keepdims=True)
    branch = hidden_grad.astype(low)
    dz_send[...] = branch
    for e in range(exps):
        total = jnp.zeros((rows, row_block), full)
        for r in range(reps):
            total = total + nt(branch[:, r * out_cols : (r + 1) * out_cols], wout[e, r])
        do_send[e] = total.astype(low)

    def do_copies():
        return [
            send(
                do_send.at[exp_peer(k)],
                do_in.at[at.exp],
                do_sem.at[SEND, exp_peer(k)],
                do_sem.at[RECV, at.exp],
                at.device(at.rep, exp_peer(k)),
            )
            for k in range(1, exps)
        ]

    for copy in do_copies():
        copy.start()
    pltpu.make_async_copy(do_send.at[at.exp], do_in.at[at.exp], do_sem.at[RECV, at.exp]).start()

    group_dz = Group(at, dz_send, dz_all, dz_sem)
    group_dz.start()
    dz_all[at.exp] = branch
    ys.start(0)
    homes[2].start()

    bias_sum[...] = jnp.zeros_like(bias_sum)

    def dn1_copies():
        beside, across = turn(at.exp, 2), turn(at.exp, 1)
        return [
            functools.partial(
                send, dn1_send.at[k], dn1_in.at[j], dn1_sem.at[SEND, j], dn1_sem.at[RECV, j], at.device(at.rep, to)
            )
            for k, j, to in ((turn(at.exp, 0), 2, beside), (across, 0, across), (beside, 1, beside))
        ]

    def attend_back(i, _):
        s = turn(at.exp, i)
        @pl.when(i == 1)
        def _():
            group_dz.pass_on()

        arrived(do_in.at[s], do_sem.at[RECV, s])
        ok = lane_of((rows, rows)) < lengths[at.base + s]
        block_lane = lane_of((rows, block_cols))
        for c in range(head_cols // block_cols):
            cols = slice(c * block_cols, (c + 1) * block_cols)
            k_cols = slice(head_cols + c * block_cols, head_cols + (c + 1) * block_cols)
            v_cols = slice(2 * head_cols + c * block_cols, 2 * head_cols + (c + 1) * block_cols)
            q = qkv[s, :, cols] * scale
            k = qkv[s, :, k_cols]
            v = qkv[s, :, v_cols]
            do = do_in[s, :, cols]
            dq = jnp.zeros((rows, block_cols), full)
            dk = jnp.zeros((rows, block_cols), full)
            dv = jnp.zeros((rows, block_cols), full)
            for t in range(block_cols // head_dim):
                h = c * (block_cols // head_dim) + t
                here = jnp.logical_and(block_lane >= t * head_dim, block_lane < (t + 1) * head_dim)
                zero = jnp.zeros_like(q)
                q_h = jnp.where(here, q, zero)
                do_h = jnp.where(here, do, zero)
                scores = nt(q_h, k) + bias[h]
                p = jnp.where(ok, jnp.exp(scores - lse[s, :, h : h + 1]), 0.0)
                dp = nt(do_h, v)
                delta = jnp.sum(dp * p, axis=1, keepdims=True)
                ds = (p * (dp - delta)).astype(low)
                bias_sum[h] += ds.astype(full)
                dv = jnp.where(here, tn(p.astype(low), do), dv)
                dq = jnp.where(here, jnp.dot(ds, k, preferred_element_type=full), dq)
                dk = jnp.where(here, tn(ds, q), dk)
            dqkv[:, cols] = (dq * scale).astype(low)
            dqkv[:, k_cols] = dk.astype(low)
            dqkv[:, v_cols] = dv.astype(low)
        dqkv_t[:, pl.ds(pl.multiple_of(s * rows, rows), rows)] = dqkv[...].T
        for e in range(exps):
            dn1_send[s, :, e * row_block : (e + 1) * row_block] = jnp.dot(
                dqkv[...], wqkv[e], preferred_element_type=full
            ).astype(low)

        @pl.when(i == 0)
        def _():
            dn1_copies()[0]().start()

        @pl.when(i == 1)
        def _():
            arrived(dn1_in.at[2], dn1_sem.at[RECV, 2])
            dn1_send[s] = (dn1_send[s].astype(full) + dn1_in[2].astype(full)).astype(low)
            dn1_copies()[1]().start()

        @pl.when(i == 2)
        def _():
            dn1_copies()[2]().start()

        return 0

    lax.fori_loop(0, exps, attend_back, 0)

    n1_copy.wait()
    seg = wq_send.shape[2]
    parts = wq_send.shape[1]
    segs = mids.shape[1] - 1
    for e in range(exps):
        part = kept[0:exps, :, e * row_block : (e + 1) * row_block].reshape(exps * rows, row_block)
        total = dot(dqkv_t[...], part)
        for j in range(parts):
            wq_send[e, j] = total[j * seg : (j + 1) * seg].astype(low)

    def owner(j):
        section, within = j // (head_cols // seg), j % (head_cols // seg)
        col = section * width + at.exp * head_cols + within * seg
        block = col // seg
        return block // segs, block % segs

    def mid_place(grp, k, quad):
        return (grp * (segs + 1) + k) * QUAD + quad

    def mid_copy(src, send_sem, rep, k, e):
        dst = mids.at[rep // QUAD, k, at.quad]
        recv = mid_sem.at[mid_place(rep // QUAD, k, at.quad)]
        stays = jnp.logical_and(rep % QUAD == at.quad, e == at.exp)
        return (
            stays,
            functools.partial(send, src, dst, send_sem, recv, (at.grp, rep % QUAD, e)),
            functools.partial(pltpu.make_async_copy, src, dst, recv),
        )

    def wq_copy(i):
        e, j = i // parts, i % parts
        rep, k = owner(j)
        return mid_copy(wq_send.at[e, j], wq_sem.at[i], rep, k, e)

    def og_copy(r):
        return mid_copy(og_send.at[r], og_sem.at[r], r, segs, at.exp)

    def go(copies, act, act_local):
        stays, away, local = copies

        @pl.when(jnp.logical_not(stays))
        def _():
            act(away)

        if act_local:

            @pl.when(stays)
            def _():
                act_local(local)

    def over(count, copies, act, act_local):
        def one(i, _):
            go(copies(i), act, act_local)
            return 0

        lax.fori_loop(0, count, one, 0)

    over(exps * parts, wq_copy, lambda copy: copy().start(), lambda copy: copy().start())
    group_dz.arrive()
    grad = tn(mine[...].reshape(exps * rows, head_cols), dz_all[...].reshape(exps * rows, width))
    for r in range(reps):
        og_send[r] = grad[:, r * out_cols : (r + 1) * out_cols].T.astype(low)
    over(reps, og_copy, lambda copy: copy().start(), lambda copy: copy().start())

    n1_grad = dn1_send[at.exp].astype(full)
    for j in range(2):
        arrived(dn1_in.at[j], dn1_sem.at[RECV, j])
        n1_grad = n1_grad + dn1_in[j].astype(full)
    x = tokens[...].astype(full)
    r1 = lax.rsqrt(jnp.mean(x * x, axis=1, keepdims=True) + eps_norm)
    scaled = n1_grad * gains[0:1, :]
    token_grad[...] = (
        dh1[...] + r1 * scaled - x * (r1 * r1 * r1) * jnp.mean(scaled * x, axis=1, keepdims=True)
    )
    small_send[exps : exps + 1, :] = jnp.sum(n1_grad * x * r1, axis=0, keepdims=True)

    line_lane = lane_of((8, 128))
    line_row = row_of((8, 128))
    bias_line = jnp.zeros((8, 128), full)
    flip = jnp.where(row_of((rows, rows)) + lane_of((rows, rows)) == rows - 1, 1.0, 0.0).astype(low)
    turned_bucket = bucket_of(rows - 1 - lane_of((8, span)))
    for h in range(heads):
        high = bias_sum[h].astype(low)
        rest = (bias_sum[h] - high.astype(full)).astype(low)
        flipped = dot(high, flip) + dot(rest, flip)
        square = jnp.concatenate([flipped, jnp.zeros((rows, rows), full)], axis=1)
        turned = pltpu.roll(square, 0, 1, stride=1, stride_axis=0)
        sums = jnp.broadcast_to(jnp.sum(turned, axis=0, keepdims=True), (8, span))
        for b in range(BUCKETS):
            value = jnp.sum(jnp.where(turned_bucket == b, sums, 0.0), axis=1, keepdims=True)
            bias_line = jnp.where(jnp.logical_and(line_row == h, line_lane == b), value, bias_line)
    for h in range(heads):
        small_send[exps + 2 : exps + 3, h * 128 : (h + 1) * 128] = bias_line[h : h + 1, :]

    def small_copies():
        return [
            send(
                small_send,
                small_exp.at[at.exp],
                small_sem.at[SEND, exp_peer(k)],
                small_sem.at[RECV, at.exp],
                at.device(at.rep, exp_peer(k)),
            )
            for k in range(1, exps)
        ]

    for copy in small_copies():
        copy.start()
    small_exp[at.exp] = small_send[...]
    ys.next(0)

    def mid_sum(grp, k):
        for q in range(QUAD):
            arrived(mids.at[grp, k, q], mid_sem.at[mid_place(grp, k, q)])
        total = mids[grp, k, 0].astype(full)
        for q in range(1, QUAD):
            total = total + mids[grp, k, q].astype(full)
        return total

    far = 1 - at.grp
    for k in range(segs + 1):
        far_send[k] = mid_sum(far, k).astype(low)

    def far_copy():
        return send(far_send, far_in, far_sem.at[SEND], far_sem.at[RECV], (far, at.quad, at.exp))

    far_copy().start()
    ys.next(1)
    for k in range(1, exps):
        arrived(small_exp.at[exp_peer(k)], small_sem.at[RECV, exp_peer(k)])
    total = small_exp[0]
    for e in range(1, exps):
        total = total + small_exp[e]
    small_sum[0] = total
    for e in range(exps):
        small_sum[0, exps + 3 + e : exps + 4 + e, :] = small_exp[e, exps + 2 : exps + 3, :]

    def small2_copies():
        return [
            send(
                small_sum.at[0],
                small_rep.at[at.rep],
                small2_sem.at[SEND, (at.rep + k) % reps],
                small2_sem.at[RECV, at.rep],
                at.device((at.rep + k) % reps, at.exp),
            )
            for k in range(1, reps)
        ]

    for copy in small2_copies():
        copy.start()
    small_rep[at.rep] = small_sum[0]
    for step in range(2, steps):
        ys.next(step)
    length = lengths[at.base]
    for e in range(1, exps):
        length = jnp.where(deal[at.base + e] == at.me, lengths[at.base + e], length)
    block = ys.result()[0]
    block_out[...] = jnp.where(row_of((rows, 1)) < length, block, jnp.zeros_like(block))
    for k in range(1, reps):
        arrived(small_rep.at[(at.rep + k) % reps], small2_sem.at[RECV, (at.rep + k) % reps])
    total = small_rep[0]
    for r in range(1, reps):
        total = total + small_rep[r]
    small_out[...] = total

    near = [mid_sum(at.grp, k) for k in range(segs + 1)]
    arrived(far_in, far_sem.at[RECV])
    grads = [(near[k] + far_in[k].astype(full)).T for k in range(segs + 1)]
    qkv_grad[...] = jnp.concatenate(grads[:segs], axis=1)
    out_grad[...] = grads[segs]
    for home in homes:
        home.arrive()

    def sent_c(k, _):
        c_copy(k)[1].wait_send()
        return 0

    lax.fori_loop(1, members, sent_c, 0)
    dn.finish()
    ys.finish()

    for home in homes:
        home.sent()

    over(exps * parts, wq_copy, lambda copy: copy().wait_send(), None)
    over(reps, og_copy, lambda copy: copy().wait_send(), None)
    far_copy().wait_send()
    for copies in (do_copies(), small_copies(), small2_copies()):
        for copy in copies:
            copy.wait_send()
    for copy in dn1_copies():
        copy().wait_send()
    group_dz.sent()


def routed(routes_t, seq, rows):
    pair = routes_t[:, pl.ds(pl.multiple_of(seq * rows, rows), rows)].astype(full)
    cols = jnp.concatenate([pair, jnp.zeros((126, rows), full)], axis=0).T
    lane = lane_of((rows, 128)).astype(full)
    return jnp.logical_or(lane == cols[:, 0:1], lane == cols[:, 1:2])


def backward_call(
    grps, exps, lengths, deal, bias_table, n_half, y_half, n_far, y_far, c_parts, both_g, down_g, in_before, down_before, n1,
    cot_all, routes_t, tokens, n2, probs, h1, qkv, lse, mine, wqkv, wout, gains, router
):
    reps = grps * QUAD
    rows, width = tokens.shape
    heads = HEADS // exps
    head_cols = width // exps
    row_block = wqkv.shape[2]
    out_cols = wout.shape[3]
    shard_cols = 3 * width // reps
    seg = math.gcd(shard_cols, head_cols)
    segs = shard_cols // seg
    parts = 3 * head_cols // seg
    members = QUAD * exps
    chip_bits = bits_of(members) - 1
    small_rows = -(-(2 * exps + 3) // 8) * 8
    shape = jax.ShapeDtypeStruct
    vmem = pl.BlockSpec(memory_space=pltpu.VMEM)
    smem = pl.BlockSpec(memory_space=pltpu.SMEM)
    hbm = pl.BlockSpec(memory_space=pl.ANY)
    results = [
        (shape((rows, width), full), vmem),
        (shape((rows, width), low), vmem),
        (shape(in_before.shape, low), hbm),
        (shape(down_before.shape, low), hbm),
        (shape((row_block, shard_cols), full), vmem),
        (shape((row_block, out_cols), full), vmem),
        (shape((small_rows, width), full), vmem),
    ]
    dma = pltpu.SemaphoreType.DMA
    bufs = [pltpu.VMEM((1 << (chip_bits - s), rows, width), low) for s in range(chip_bits + 1)]
    return pl.pallas_call(
        functools.partial(backward_kernel, grps, exps),
        out_shape=[r[0] for r in results],
        in_specs=[smem] * 3 + [hbm] * 11 + [vmem] * 4 + [hbm] * 6 + [vmem] * 2,
        out_specs=[r[1] for r in results],
        scratch_shapes=[
            pltpu.VMEM(h1.shape, full),
            pltpu.VMEM(qkv.shape, low),
            pltpu.VMEM(lse.shape, full),
            pltpu.VMEM(mine.shape, low),
            pltpu.VMEM(wqkv.shape, low),
            pltpu.VMEM(wout.shape, low),
            pltpu.VMEM((members // 2, rows, width), low),
            list(bufs),
            list(bufs),
            pltpu.VMEM((members, 8, rows), full),
            pltpu.VMEM((rows, width), full),
            pltpu.VMEM((rows, width), low),
            pltpu.VMEM((exps, rows, width), low),
            pltpu.VMEM((exps, rows, head_cols), low),
            pltpu.VMEM((exps, rows, head_cols), low),
            pltpu.VMEM((heads, rows, rows), full),
            pltpu.VMEM((heads, rows, rows), full),
            pltpu.VMEM((rows, 3 * head_cols), low),
            pltpu.VMEM((3 * head_cols, exps * rows), low),
            pltpu.VMEM((exps, rows, width), low),
            pltpu.VMEM((3, rows, width), low),
            pltpu.VMEM((exps, parts, seg, row_block), low),
            pltpu.VMEM((reps, seg, row_block), low),
            pltpu.VMEM((grps, segs + 1, QUAD, seg, row_block), low),
            pltpu.VMEM((segs + 1, seg, row_block), low),
            pltpu.VMEM((segs + 1, seg, row_block), low),
            pltpu.VMEM((small_rows, width), full),
            pltpu.VMEM((exps, small_rows, width), full),
            pltpu.VMEM((1, small_rows, width), full),
            pltpu.VMEM((reps, small_rows, width), full),
            dma((2, 3 << chip_bits)),
            dma((2, 3 << chip_bits)),
            dma((2, 2, members // 2)),
            dma((2, members)),
            dma((3, 2, 2 * reps)),
            dma((3, 2, max(QUAD, grps))),
            dma((2, exps)),
            dma((2, exps)),
            dma((2, exps)),
            dma((exps * parts,)),
            dma((reps,)),
            dma((grps * (segs + 1) * QUAD,)),
            dma((2,)),
            dma((2, exps)),
            dma((2, reps)),
            dma((2,)),
            dma((6,)),
        ],
        compiler_params=pltpu.CompilerParams(
            collective_id=1, has_side_effects=True, vmem_limit_bytes=60 * 1024 * 1024
        ),
        input_output_aliases={10: 2, 11: 3},
        name="backward",
    )(
        lengths, deal, bias_table, n_half, y_half, n_far, y_far, c_parts, both_g, down_g, in_before, down_before, n1, cot_all,
        routes_t, tokens, n2, probs, h1, qkv, lse, mine, wqkv, wout, gains, router
    )


def per_device(
    tokens,
    cotangent,
    seq_lengths,
    deal,
    routes,
    attn_qkv,
    qkv_first,
    qkv_second,
    attn_out,
    out_first,
    out_second,
    rel_bias,
    bias_first,
    bias_second,
    router,
    router_first,
    router_second,
    norm_gains,
    gains_first,
    gains_second,
    expert_in,
    in_first,
    in_second,
    expert_out,
    down_first,
    down_second,
):
    rows, width = tokens.shape
    experts = router.shape[1]
    capacity = (10 * rows + 4 * experts - 1) // (4 * experts)
    exps = lax.axis_size("exp")
    grps = lax.axis_size("grp")
    routes_t = routes.T
    bias_table = rel_bias.T
    (
        both_w, down_w, cot_all, n_all, comb_all, qkv, lse, context_mine, normed_group, wqkv, wout, hidden_one,
        normed_two, router_probs, in_low, down_low,
    ) = forward_call(
        grps, exps, seq_lengths, bias_table, routes_t, tokens, cotangent, norm_gains.T, router.T,
        attn_qkv, attn_out, expert_in[0], expert_out[0],
    )
    n_half, y_half, n_far, y_far, c_parts, both_g, down_g, in_before, down_before = expert_call(
        grps, exps, capacity, deal, routes_t, comb_all, n_all, cot_all, both_w, down_w, in_low, down_low,
        hidden_one,
    )
    token_grad, block_out, in_parts, down_parts, qkv_grad, out_grad, small = backward_call(
        grps, exps, seq_lengths, deal, bias_table, n_half, y_half, n_far, y_far, c_parts, both_g, down_g,
        in_before, down_before, normed_group, cot_all, routes_t, tokens, normed_two, router_probs, hidden_one, qkv, lse, context_mine, wqkv,
        wout, norm_gains.T, router.T,
    )
    states = [
        attn_qkv, qkv_first, qkv_second, attn_out, out_first, out_second, bias_table, bias_first.T, bias_second.T,
        router.T, router_first.T, router_second.T, norm_gains.T, gains_first.T, gains_second.T,
        expert_in[0], in_first[0], in_second[0], expert_out[0], down_first[0], down_second[0],
    ]
    new = list(adam_call(exps, in_parts, down_parts, qkv_grad, out_grad, small, states))
    new = new[:6] + [array.T for array in new[6:15]] + [array[None] for array in new[15:]]
    return (block_out, token_grad, *new)


def bucket_onehot(length):
    places = jnp.arange(length, dtype=jnp.int32)
    offset = places[None, :] - places[:, None]
    distance = jnp.abs(offset)
    bucket = 16 * (offset > 0).astype(jnp.int32)
    for threshold in thresholds:
        bucket = bucket + (distance >= threshold).astype(jnp.int32)
    return (bucket[:, :, None] == jnp.arange(BUCKETS, dtype=jnp.int32)[None, None, :]).astype(full)


def swap(pieces, axes):
    return lax.all_to_all(pieces, axes, split_axis=0, concat_axis=0, tiled=True)


def spread(block, axes):
    members = lax.axis_size(axes)
    return swap(jnp.broadcast_to(block[None], (members,) + block.shape), axes)


def plain_device(
    tokens,
    cotangent,
    seq_lengths,
    deal,
    routes,
    attn_qkv,
    qkv_first,
    qkv_second,
    attn_out,
    out_first,
    out_second,
    rel_bias,
    bias_first,
    bias_second,
    router,
    router_first,
    router_second,
    norm_gains,
    gains_first,
    gains_second,
    expert_in,
    in_first,
    in_second,
    expert_out,
    down_first,
    down_second,
):
    rows, width = tokens.shape
    head_dim = width // HEADS
    score_scale = 1.0 / math.sqrt(head_dim)
    experts = router.shape[1]
    capacity = (10 * rows + 4 * experts - 1) // (4 * experts)
    exps = lax.axis_size("exp")
    grps = lax.axis_size("grp")
    reps = grps * QUAD
    heads = HEADS // exps
    head_cols = heads * head_dim
    place = lax.axis_index("exp")
    base = lax.axis_index(REP) * exps
    me = base + place
    slab = expert_in.shape[1]
    units = expert_out.shape[1]
    quarter = grps * units

    row_block = attn_qkv.shape[0]
    qkv_rows = lax.all_gather(attn_qkv.astype(low), REP, axis=1, tiled=True)
    out_rows = lax.all_gather(attn_out.astype(low), REP, axis=1, tiled=True)
    qkv_pieces = jnp.transpose(
        qkv_rows.reshape(row_block, 3, exps, head_cols), (2, 0, 1, 3)
    ).reshape(exps, row_block, 3 * head_cols)
    qkv_mine = swap(qkv_pieces, "exp").reshape(width, 3 * head_cols)
    full_out = spread(out_rows, "exp").reshape(width, width)

    group_tokens = spread(tokens, "exp")
    group_cotangent = spread(cotangent, "exp")
    my_cotangent = lax.dynamic_index_in_dim(group_cotangent, deal[me] - base, 0, keepdims=False)

    my_routes = lax.dynamic_slice_in_dim(routes, me * rows, rows, 0)
    places = jnp.arange(rows, dtype=jnp.int32)
    valid_rows = (places < seq_lengths[me]).astype(full)
    group_lengths = lax.dynamic_slice_in_dim(seq_lengths, base, exps, 0)
    key_ok = places[None, :] < group_lengths[:, None]
    gain_one = norm_gains[:, 0]
    gain_two = norm_gains[:, 1]

    chosen = (my_routes[:, :, None] == jnp.arange(experts, dtype=jnp.int32)[None, None, :]).astype(full)
    flat_routes = my_routes.reshape(-1)
    route_hot = (flat_routes[:, None] == jnp.arange(experts, dtype=jnp.int32)[None, :]).astype(jnp.int32)
    before = jnp.cumsum(route_hot, axis=0) - route_hot
    slot_index = jnp.sum(before * route_hot, axis=-1)
    target = (flat_routes * capacity + slot_index).reshape(rows, 2)
    slots = experts * capacity
    slot_ids = jnp.arange(slots, dtype=jnp.int32)
    place_first = slot_ids[:, None] == target[None, :, 0]
    place_second = slot_ids[:, None] == target[None, :, 1]
    place_any = jnp.logical_or(place_first, place_second).astype(low)

    shard_in = expert_in[0].astype(low).reshape(slab, 2, grps, QUAD, units)
    in_pieces = jnp.transpose(shard_in, (1, 3, 0, 2, 4)).reshape(2, 1, QUAD, slab, quarter)
    in_pieces = jnp.broadcast_to(in_pieces, (2, grps, QUAD, slab, quarter)).reshape(
        2, reps, slab, quarter
    )
    down_mine = spread(expert_out[0].astype(low), "grp").reshape(quarter, width)
    gate_mine = swap(in_pieces[0], REP).reshape(width, quarter)
    up_mine = swap(in_pieces[1], REP).reshape(width, quarter)

    upstream = my_cotangent.astype(full) * valid_rows[:, None]

    def to_experts(block):
        sent = block.reshape((1, experts) + block.shape[1:])
        sent = jnp.broadcast_to(sent, (QUAD,) + sent.shape[1:])
        return swap(sent.reshape((QUAD * experts,) + block.shape[1:]), PLANE)

    def dispatch(values):
        return dot(place_any, values).astype(low).reshape(experts, capacity, width)

    expert_upstream = to_experts(dispatch(upstream.astype(low))).reshape(-1, width)
    active_grad_bare = lax.dot_general(
        expert_upstream, down_mine, (((1,), (1,)), ((), ())), preferred_element_type=full
    )

    x_group = group_tokens.astype(full)
    scale_group = lax.rsqrt(jnp.mean(x_group * x_group, axis=-1, keepdims=True) + eps_norm)
    normed_group = (x_group * scale_group * gain_one).astype(low).reshape(exps * rows, width)
    qkv = dot(normed_group, qkv_mine).astype(low).reshape(exps, rows, 3, heads, head_dim)
    queries = qkv[:, :, 0]
    key_rows = qkv[:, :, 1]
    values = qkv[:, :, 2]
    onehot = bucket_onehot(rows)
    bias_mine = lax.dynamic_slice_in_dim(rel_bias, place * heads, heads, 1)
    bias_table = jnp.einsum("ijb,bh->hij", onehot, bias_mine, precision=highest)

    def scores_of():
        raw = (
            jnp.einsum("sihd,sjhd->shij", queries, key_rows, preferred_element_type=full)
            * score_scale
            + bias_table[None]
        )
        return jnp.where(key_ok[:, None, None, :], raw, -1e30)

    scores = scores_of()
    row_max = jnp.max(scores, axis=-1, keepdims=True)
    log_total = row_max + jnp.log(jnp.sum(jnp.exp(scores - row_max), axis=-1, keepdims=True))
    weights_low = jnp.exp(scores - log_total).astype(low)
    context_mine = (
        jnp.einsum("shij,sjhd->sihd", weights_low, values, preferred_element_type=full)
        .astype(low)
        .reshape(exps, rows, head_cols)
    )
    context = jnp.transpose(swap(context_mine, "exp"), (1, 0, 2)).reshape(rows, width)

    x_float = tokens.astype(full)
    scale_one = lax.rsqrt(jnp.mean(x_float * x_float, axis=-1, keepdims=True) + eps_norm)
    hidden_one = x_float + dot(context, full_out)
    scale_two = lax.rsqrt(jnp.mean(hidden_one * hidden_one, axis=-1, keepdims=True) + eps_norm)
    normed_two = (hidden_one * scale_two * gain_two).astype(low)
    normed_float = normed_two.astype(full)
    router_probs = jax.nn.softmax(jnp.dot(normed_float, router, precision=highest), axis=-1)
    picked = jnp.sum(router_probs[:, None, :] * chosen, axis=-1)
    gate_total = jnp.sum(picked, axis=-1, keepdims=True)
    gate_value = picked / gate_total
    combine = gate_value * valid_rows[:, None]
    combine_slots = jnp.sum(
        jnp.where(place_first, combine[None, :, 0], 0.0)
        + jnp.where(place_second, combine[None, :, 1], 0.0),
        axis=1,
    ).reshape(experts, 1, capacity)

    expert_rows = to_experts(dispatch(normed_two)).reshape(-1, width)
    expert_combine = to_experts(combine_slots).reshape(-1, 1)

    gate_part = dot(expert_rows, gate_mine)
    up_part = dot(expert_rows, up_mine)
    active_float, active_pull = jax.vjp(gated_unit, gate_part, up_part)
    active = active_float.astype(low)
    active_scaled = (active_float * expert_combine).astype(low)
    combine_grad_part = jnp.sum(active_float * active_grad_bare, axis=-1).reshape(
        QUAD * experts, 1, capacity
    )
    gate_part_grad, up_part_grad = active_pull(active_grad_bare * expert_combine)
    gate_part_grad = gate_part_grad.astype(low)
    up_part_grad = up_part_grad.astype(low)
    rows_grad_part = (
        lax.dot_general(gate_part_grad, gate_mine, (((1,), (1,)), ((), ())), preferred_element_type=full)
        + lax.dot_general(up_part_grad, up_mine, (((1,), (1,)), ((), ())), preferred_element_type=full)
    ).astype(low)
    output_part = dot(active, down_mine).astype(low)

    combine_grad_back = swap(combine_grad_part, PLANE)
    rows_grad_back = swap(rows_grad_part.reshape(QUAD * experts, capacity, width), PLANE)
    output_back = swap(output_part.reshape(QUAD * experts, capacity, width), PLANE)

    def transposed_dot(a, b):
        return lax.dot_general(a, b, (((0,), (0,)), ((), ())), preferred_element_type=full)

    down_grad = transposed_dot(active_scaled, expert_upstream).astype(low)
    gate_grad = transposed_dot(expert_rows, gate_part_grad).astype(low)
    up_grad = transposed_dot(expert_rows, up_part_grad).astype(low)
    down_share = jnp.sum(
        swap(down_grad.reshape(grps, units, width), "grp").astype(full), axis=0
    )[None]

    def in_columns(grad):
        back = swap(grad.reshape(reps, slab, quarter), REP).astype(full)
        back = jnp.sum(back.reshape(grps, QUAD, slab, grps, units), axis=0)
        return jnp.transpose(back, (1, 2, 0, 3)).reshape(slab, grps * QUAD * units)

    in_share = jnp.concatenate([in_columns(gate_grad), in_columns(up_grad)], axis=1)[None]

    def from_slots(placed, parts):
        hot = jnp.broadcast_to(placed.astype(low)[None], (QUAD,) + placed.shape).reshape(-1, rows)
        return lax.dot_general(
            hot, parts.reshape(-1, width), (((0,), (0,)), ((), ())), preferred_element_type=full
        )

    mixture = combine[:, :1] * from_slots(place_first, output_back) + combine[:, 1:] * from_slots(
        place_second, output_back
    )
    block_loader = (valid_rows[:, None] * (hidden_one + mixture)).astype(low)
    seq_ids = jnp.arange(deal.shape[0], dtype=jnp.int32)
    dealt_seq = jnp.sum(jnp.where(deal == me, seq_ids, 0))
    block_out = lax.dynamic_index_in_dim(
        spread(block_loader, "exp"), dealt_seq - base, 0, keepdims=False
    )

    combine_grad_slots = jnp.sum(combine_grad_back.reshape(QUAD, slots), axis=0)
    combine_grad = jnp.stack(
        [
            jnp.sum(jnp.where(place_first, combine_grad_slots[:, None], 0.0), axis=0),
            jnp.sum(jnp.where(place_second, combine_grad_slots[:, None], 0.0), axis=0),
        ],
        axis=1,
    )
    gate_grad_value = combine_grad * valid_rows[:, None]
    picked_grad = (
        gate_grad_value - jnp.sum(gate_grad_value * gate_value, axis=-1, keepdims=True)
    ) / gate_total
    probs_grad = jnp.sum(picked_grad[:, :, None] * chosen, axis=1)
    logit_grad = router_probs * (
        probs_grad - jnp.sum(probs_grad * router_probs, axis=-1, keepdims=True)
    )
    router_grad = jnp.dot(normed_float.T, logit_grad, precision=highest)
    normed_grad = jnp.dot(logit_grad, router.T, precision=highest) + from_slots(
        jnp.logical_or(place_first, place_second), rows_grad_back
    )
    scaled_two = normed_grad * gain_two
    hidden_grad = (
        upstream
        + scale_two * scaled_two
        - hidden_one * scale_two**3 * jnp.mean(scaled_two * hidden_one, axis=-1, keepdims=True)
    )
    gain_two_grad = jnp.sum(normed_grad * hidden_one * scale_two, axis=0)
    branch_grad = hidden_grad.astype(low)
    context_grad = lax.dot_general(
        branch_grad, full_out, (((1,), (1,)), ((), ())), preferred_element_type=full
    ).astype(low)
    context_grad_pieces = jnp.transpose(context_grad.reshape(rows, exps, head_cols), (1, 0, 2))
    context_grad_mine = swap(context_grad_pieces, "exp").reshape(exps, rows, heads, head_dim)
    branch_group = spread(branch_grad, "exp").reshape(exps * rows, width)
    out_grad = transposed_dot(context_mine.reshape(exps * rows, head_cols), branch_group).astype(low)

    scores = scores_of()
    probs_again = jnp.exp(scores - log_total)
    weights_again = probs_again.astype(low)
    values_grad = jnp.einsum(
        "shij,sihd->sjhd", weights_again, context_grad_mine, preferred_element_type=full
    )
    probs_grad_att = jnp.einsum(
        "sihd,sjhd->shij", context_grad_mine, values, preferred_element_type=full
    )
    row_delta = jnp.sum(probs_grad_att * probs_again, axis=-1, keepdims=True)
    scores_grad = (probs_again * (probs_grad_att - row_delta)).astype(low)
    scores_grad_sum = jnp.sum(scores_grad.astype(full), axis=0)
    bias_grad_mine = jnp.einsum("hij,ijb->bh", scores_grad_sum, onehot, precision=highest)
    bias_grad = lax.dynamic_update_slice_in_dim(
        jnp.zeros((BUCKETS, HEADS), full), bias_grad_mine, place * heads, 1
    )
    queries_grad = (
        jnp.einsum("shij,sjhd->sihd", scores_grad, key_rows, preferred_element_type=full)
        * score_scale
    )
    keys_grad = (
        jnp.einsum("shij,sihd->sjhd", scores_grad, queries, preferred_element_type=full)
        * score_scale
    )
    qkv_grad = (
        jnp.stack([queries_grad, keys_grad, values_grad], axis=2)
        .astype(low)
        .reshape(exps * rows, 3 * head_cols)
    )
    normed_one_part = lax.dot_general(
        qkv_grad, qkv_mine, (((1,), (1,)), ((), ())), preferred_element_type=full
    ).astype(low)
    normed_one_grad = jnp.sum(
        swap(normed_one_part.reshape(exps, rows, width), "exp").astype(full), axis=0
    )
    scaled_one = normed_one_grad * gain_one
    token_grad = (
        hidden_grad
        + scale_one * scaled_one
        - x_float * scale_one**3 * jnp.mean(scaled_one * x_float, axis=-1, keepdims=True)
    )
    gain_one_grad = jnp.sum(normed_one_grad * x_float * scale_one, axis=0)

    qkv_weight_grad = transposed_dot(normed_group, qkv_grad).astype(low)
    qkv_grad_rows = swap(qkv_weight_grad.reshape(exps, row_block, 3 * head_cols), "exp")
    qkv_grad_rows = jnp.transpose(
        qkv_grad_rows.reshape(exps, row_block, 3, head_cols), (1, 2, 0, 3)
    ).reshape(row_block, reps, -1)
    qkv_share = jnp.sum(
        swap(jnp.transpose(qkv_grad_rows, (1, 0, 2)), REP).astype(full), axis=0
    )
    out_pieces = jnp.transpose(out_grad.reshape(row_block, reps, -1), (1, 0, 2))
    out_share = jnp.sum(swap(out_pieces, REP).astype(full), axis=0)

    small = jnp.concatenate(
        [
            router_grad.reshape(-1),
            jnp.stack([gain_one_grad, gain_two_grad], axis=1).reshape(-1),
            bias_grad.reshape(-1),
        ]
    ).reshape(-1, 128)
    small_total = jnp.sum(lax.all_gather(small, ALL, axis=0, tiled=False), axis=0).reshape(-1)
    router_total = small_total[: router.size].reshape(router.shape)
    gains_total = small_total[router.size : router.size + norm_gains.size].reshape(norm_gains.shape)
    bias_total = small_total[router.size + norm_gains.size :].reshape(rel_bias.shape)

    qkv_new = adamw_update(attn_qkv, qkv_first, qkv_second, qkv_share, 1.5 / math.sqrt(D), 0.1)
    out_new = adamw_update(attn_out, out_first, out_second, out_share, 6.0 / math.sqrt(D), 0.1)
    bias_new = adamw_update(rel_bias, bias_first, bias_second, bias_total, 0.3, 0.0)
    router_new = adamw_update(
        router, router_first, router_second, router_total, 1.0 / math.sqrt(D), 0.1
    )
    gains_new = adamw_update(norm_gains, gains_first, gains_second, gains_total, 0.5, 0.0)
    in_new = adamw_update(expert_in, in_first, in_second, in_share, 1.5 / math.sqrt(D), 0.1)
    down_new = adamw_update(
        expert_out, down_first, down_second, down_share, 1.5 / math.sqrt(FF), 0.1
    )
    return (
        (block_out, token_grad)
        + qkv_new
        + out_new
        + bias_new
        + router_new
        + gains_new
        + in_new
        + down_new
    )


def solution(mesh):
    reps, exps = mesh.devices.shape
    split = Mesh(mesh.devices.reshape(reps // QUAD, QUAD, exps), ALL)
    by_rows = P(ALL, None)
    attn = P("exp", REP)
    expert = P("exp", REP, None)
    return jax.shard_map(
        per_device if (reps, exps) == (2 * QUAD, 4) else plain_device,
        mesh=split,
        in_specs=(by_rows, by_rows) + (P(),) * 3 + (attn,) * 6 + (P(),) * 9 + (expert,) * 6,
        out_specs=(by_rows, by_rows) + (attn,) * 6 + (P(),) * 9 + (expert,) * 6,
        check_vma=False,
    )
```

```python
import functools
import math

import jax
import jax.numpy as jnp
from jax import lax
from jax.experimental import pallas as pl
from jax.experimental.pallas import tpu as pltpu
from jax.sharding import Mesh
from jax.sharding import PartitionSpec as P

D = 1024
HEADS = 16
FF = 2816
BUCKETS = 32
STEP = 10
QUAD = 4
REP = ("grp", "quad")
PLANE = ("quad", "exp")
ALL = ("grp", "quad", "exp")

highest = lax.Precision.HIGHEST
eps_norm = 1e-06
thresholds = (1, 2, 3, 4, 5, 6, 7, 8, 11, 16, 22, 32, 45, 64, 90)
beta_one = 0.9
beta_two = 0.999
eps_adam = 1e-08
low = jnp.bfloat16
full = jnp.float32
MESH = pl.DeviceIdType.MESH


def adamw_update(weight, moment, second, gradient, step_rate, decay_factor):
    new_moment = beta_one * moment + (1.0 - beta_one) * gradient
    new_second = beta_two * second + (1.0 - beta_two) * gradient * gradient
    corrected = new_moment / (1.0 - beta_one**STEP)
    scaled = new_second / (1.0 - beta_two**STEP)
    new_weight = weight - step_rate * (
        corrected / (jnp.sqrt(scaled) + eps_adam) + decay_factor * weight
    )
    return (new_moment, new_second, new_weight)


def gated_unit(gate_input, up_input):
    return jax.nn.gelu(gate_input, approximate=True) * up_input


def dot(a, b):
    return jnp.dot(a, b, preferred_element_type=full)


def nt(a, b, precision=None):
    return lax.dot_general(a, b, (((1,), (1,)), ((), ())), preferred_element_type=full, precision=precision)


def tn(a, b):
    return lax.dot_general(a, b, (((0,), (0,)), ((), ())), preferred_element_type=full)


class Where:
    def __init__(self, grps, exps):
        self.grps, self.exps = grps, exps
        self.reps = grps * QUAD
        self.grp = lax.axis_index("grp")
        self.quad = lax.axis_index("quad")
        self.exp = lax.axis_index("exp")
        self.rep = self.grp * QUAD + self.quad
        self.base = self.rep * exps
        self.me = self.base + self.exp

    def device(self, rep, exp):
        return (rep // QUAD, rep % QUAD, exp)

    def near(self, flip):
        q = self.quad
        if flip & 1:
            q = q + 1 - 2 * (q % 2)
        if flip & 2:
            q = q + 2 - 4 * (q // 2)
        return q


def send(src, dst, send_sem, recv_sem, device):
    return pltpu.make_async_remote_copy(
        src_ref=src, dst_ref=dst, send_sem=send_sem, recv_sem=recv_sem, device_id=device, device_id_type=MESH
    )


def arrived(ref, sem):
    pltpu.make_async_copy(ref, ref, sem).wait()


def greet(at, count, device):
    barrier = pltpu.get_barrier_semaphore()

    def one(k, _):
        pl.semaphore_signal(barrier, inc=1, device_id=device(k), device_id_type=MESH)
        return 0

    lax.fori_loop(1, count + 1, one, 0)
    pl.semaphore_wait(barrier, count)


def everyone(at):
    count = at.reps * at.exps

    def device(k):
        other = (at.me + k) % count
        return at.device(other // at.exps, other % at.exps)

    return count - 1, device


def turn(exp, i):
    beside = exp + 1 - 2 * (exp % 2)
    return jnp.where(i == 0, (beside + 2) % 4, jnp.where(i == 1, (exp + 2) % 4, jnp.where(i == 2, beside, exp)))


def lane_of(shape):
    return lax.broadcasted_iota(jnp.int32, shape, 1)


def row_of(shape):
    return lax.broadcasted_iota(jnp.int32, shape, 0)


def bucket_of(offset):
    distance = jnp.abs(offset)
    bucket = jnp.where(offset > 0, 16, 0)
    for threshold in thresholds:
        bucket = bucket + jnp.where(distance >= threshold, 1, 0)
    return bucket


def bits_of(count):
    return count.bit_length() - 1


def column_parts(width):
    tiles = width // 128
    cuts = [0, (tiles + 2) // 3, (2 * tiles + 2) // 3, tiles]
    return [(cuts[i] * 128, (cuts[i + 1] - cuts[i]) * 128) for i in range(3)]


def flipped(place, bit):
    return place + (1 - 2 * ((place // (1 << bit)) % 2)) * (1 << bit)


class Doubling:
    def __init__(self, at, own, every, sems, core_sems, orders):
        self.at, self.own, self.every = at, own, every
        self.sems, self.core_sems, self.orders = sems, core_sems, orders
        self.plane = at.quad * at.exps + at.exp
        self.steps = len(orders[0])
        self.parts = column_parts(own.shape[1])

    def device(self, bit):
        other = flipped(self.plane, bit)
        return (self.at.grp, other // self.at.exps, other % self.at.exps)

    def place(self, part, j):
        p = self.plane
        for i, bit in enumerate(self.orders[part]):
            if (j >> i) & 1:
                p = flipped(p, bit + 1)
        return p

    def block(self, part, p):
        begin, size = self.parts[part]
        return self.every.at[p, :, pl.ds(begin, size)]

    def source(self, part, j):
        begin, size = self.parts[part]
        return self.own.at[:, pl.ds(begin, size)] if j == 0 else self.block(part, self.place(part, j))

    def index(self, step, part, j):
        return part * (1 << self.steps) + (1 << step) - 1 + j

    def copy(self, step, part, j):
        i = self.index(step, part, j)
        return send(
            self.source(part, j),
            self.block(part, self.place(part, j)),
            self.sems.at[0, i],
            self.sems.at[1, i],
            self.device(self.orders[part][step] + 1),
        )

    def core_copy(self, part, j):
        i = part * (1 << self.steps) + j
        return send(
            self.source(part, j),
            self.block(part, self.place(part, j)),
            self.core_sems.at[0, i],
            self.core_sems.at[1, i],
            self.device(0),
        )

    def start(self):
        for part in range(3):
            for step in range(self.steps):
                self.copy(step, part, 0).start()
        for part in range(3):
            self.core_copy(part, 0).start()
        self.keep().start()

    def keep(self):
        return pltpu.make_async_copy(self.own, self.every.at[self.plane], self.core_sems.at[1, 3 << self.steps])

    def next(self, step):
        for part in range(3):
            for j in range(1 << step):
                k = (1 << step) + j
                arrived(self.block(part, self.place(part, k)), self.sems.at[1, self.index(step, part, j)])
                for later in range(step + 1, self.steps):
                    self.copy(later, part, k).start()
                self.core_copy(part, k).start()

    def finish_in(self):
        for part in range(3):
            for j in range(1 << self.steps):
                there = self.block(part, flipped(self.place(part, j), 0))
                arrived(there, self.core_sems.at[1, part * (1 << self.steps) + j])
        self.keep().wait()

    def finish_out(self):
        for part in range(3):
            for j in range(1 << self.steps):
                self.core_copy(part, j).wait_send()
            for step in range(self.steps):
                for j in range(1 << step):
                    self.copy(step, part, j).wait_send()


class Group:
    def __init__(self, at, own, every, sems):
        self.at, self.own, self.every, self.sems = at, own, every, sems
        self.beside, self.across = at.exp + 1 - 2 * (at.exp % 2), (at.exp + 2) % 4

    def copy(self, src, index, send_index, device):
        return send(
            src, self.every.at[index], self.sems.at[0, send_index], self.sems.at[1, index], self.at.device(self.at.rep, device)
        )

    def first(self):
        return [
            self.copy(self.own, self.at.exp, 0, self.across),
            self.copy(self.own, self.at.exp, 1, self.beside),
        ]

    def second(self):
        return self.copy(self.every.at[self.across], self.across, 2, self.beside)

    def start(self):
        for copy in self.first():
            copy.start()

    def pass_on(self):
        arrived(self.every.at[self.across], self.sems.at[1, self.across])
        self.second().start()

    def arrive(self):
        for index in (self.beside, (self.beside + 2) % 4):
            arrived(self.every.at[index], self.sems.at[1, index])

    def sent(self):
        for copy in self.first() + [self.second()]:
            copy.wait_send()


class Tiles:
    def __init__(self, units, reps):
        self.units = units
        self.reps = reps
        self.hidden = units * reps
        self.half = self.hidden // 256
        self.wide = (self.half + 1) // 2
        self.count = 3
        self.size = 128 * self.wide // self.count
        self.skip = 128 * (2 * self.wide - self.half)

    def start(self, quad):
        return 128 * (self.half * (quad // 2) + (self.half - self.wide) * (quad % 2))

    def rows(self, tile):
        result = []
        for k in range(QUAD):
            found = None
            for parity in range(2):
                first = self.start(parity) + tile * self.size
                live = first + (self.skip if parity and tile == 0 else 0)
                begin = max(live, k * self.units)
                end = min(first + self.size, (k + 1) * self.units)
                if end > begin:
                    found = (begin - k * self.units, end - begin, parity, begin - first)
            result.append(found)
        return result


class Outward:
    def __init__(self, at, tiles, tile, in_low, down_slab, both_w, down_w, nothing, sems, down_sems):
        self.at, self.tiles, self.tile = at, tiles, tile
        self.in_low, self.down_slab, self.both_w, self.down_w = in_low, down_slab, both_w, down_w
        self.nothing, self.sems, self.down_sems = nothing, sems, down_sems
        self.slab = in_low.shape[0]

    def source(self, quad, section):
        begin = section * self.tiles.hidden + self.tiles.start(quad) + self.tile * self.tiles.size
        return self.in_low.at[:, pl.ds(pl.multiple_of(begin, 128), self.tiles.size)]

    def target(self, rep, section):
        rows = pl.ds(pl.multiple_of(rep * self.slab, self.slab), self.slab)
        return self.both_w.at[rows, pl.ds(section * self.tiles.size, self.tiles.size)]

    def over(self, act):
        at = self.at

        def one(k, _):
            other = (at.rep + k) % at.reps
            for section in range(2):
                act(
                    functools.partial(
                        send,
                        self.source(other % QUAD, section),
                        self.target(at.rep, section),
                        self.sems.at[0, section * at.reps + other],
                        self.sems.at[1, section * at.reps + at.rep],
                        at.device(other, at.exp),
                    )
                )
            return 0

        lax.fori_loop(1, at.reps, one, 0)

    def over_down(self, act, act_local):
        at = self.at
        for k, piece in enumerate(self.tiles.rows(self.tile)):
            if piece is None:
                continue
            begin, count, parity, to = piece
            quad = 2 * (at.rep // QUAD) + parity
            src, dst = self.down_slab.at[pl.ds(begin, count)], self.down_w.at[pl.ds(to, count)]
            recv = self.down_sems.at[1, at.rep]
            for g in range(at.grps):
                stays = jnp.logical_and(at.grp == g, at.quad == quad)
                ours = at.rep % QUAD == k

                @pl.when(jnp.logical_and(ours, jnp.logical_not(stays)))
                def _():
                    act(functools.partial(send, src, dst, self.down_sems.at[0, g], recv, (g, quad, at.exp)))

                @pl.when(jnp.logical_and(ours, stays))
                def _():
                    act_local(functools.partial(pltpu.make_async_copy, src, dst, recv))

    def blank(self):
        return pltpu.make_async_copy(
            self.nothing, self.down_w.at[pl.ds(0, self.tiles.skip)], self.down_sems.at[1, self.at.reps]
        )

    def start(self):
        at = self.at
        self.over_down(lambda copy: copy().start(), lambda copy: copy().start())
        self.over(lambda copy: copy().start())
        for section in range(2):
            pltpu.make_async_copy(
                self.source(at.quad, section), self.target(at.rep, section), self.sems.at[1, section * at.reps + at.rep]
            ).start()
        if self.tile == 0:

            @pl.when(at.quad % 2 == 1)
            def _():
                self.blank().start()

    def arrive(self):
        at = self.at

        def one(rep, _):
            for section in range(2):
                arrived(self.target(rep, section), self.sems.at[1, section * at.reps + rep])
            return 0

        lax.fori_loop(0, at.reps, one, 0)
        for parity in range(2):

            @pl.when(at.quad % 2 == parity)
            def _():
                for k, piece in enumerate(self.tiles.rows(self.tile)):
                    if piece is not None and piece[2] == parity:
                        source = QUAD * (at.quad // 2) + k
                        arrived(self.down_w.at[pl.ds(piece[3], piece[1])], self.down_sems.at[1, source])
                if parity and self.tile == 0:
                    self.blank().wait()

    def sent(self):
        self.over(lambda copy: copy().wait_send())
        self.over_down(lambda copy: copy().wait_send(), lambda copy: None)


class Homeward:
    def __init__(self, at, tiles, tile, both, down, in_parts, down_parts, sems, down_sems, sections=(0, 1)):
        self.at, self.tiles, self.tile, self.sections = at, tiles, tile, sections
        self.both, self.down, self.in_parts, self.down_parts = both, down, in_parts, down_parts
        self.sems, self.down_sems = sems, down_sems
        self.slab = in_parts.shape[1]

    def target(self, grp, quad, parity, section):
        skip = self.tiles.skip if parity and self.tile == 0 else 0
        to = section * self.tiles.hidden + self.tiles.start(quad) + self.tile * self.tiles.size + skip
        to = to if isinstance(to, int) else pl.multiple_of(to, 128)
        return skip, self.in_parts.at[grp, :, pl.ds(to, self.tiles.size - skip)]

    def copy(self, rep, parity, section, local=False):
        at = self.at
        skip, dst = self.target(at.grp, at.quad, parity, section)
        rows = pl.ds(pl.multiple_of(rep * self.slab, self.slab), self.slab)
        src = self.both.at[rows, pl.ds(section * self.tiles.size + skip, self.tiles.size - skip)]
        recv = self.sems.at[1, section * at.reps + at.rep]
        if local:
            return pltpu.make_async_copy(src, dst, recv)
        return send(src, dst, self.sems.at[0, section * at.reps + rep], recv, at.device(rep, at.exp))

    def over(self, act, act_local):
        at = self.at
        for parity in range(2):

            @pl.when(at.quad % 2 == parity)
            def _():
                def one(k, _):
                    for section in self.sections:
                        act(self.copy((at.rep + k) % at.reps, parity, section))
                    return 0

                lax.fori_loop(1, at.reps, one, 0)
                if act_local:
                    for section in self.sections:
                        act_local(self.copy(at.rep, parity, section, local=True))

    def over_down(self, act, act_local):
        at = self.at
        if self.down is None:
            return
        for k, piece in enumerate(self.tiles.rows(self.tile)):
            if piece is None:
                continue
            begin, count, parity, to = piece
            src, dst = self.down.at[pl.ds(to, count)], self.down_parts.at[at.grp, pl.ds(begin, count)]
            recv = self.down_sems.at[1, at.grp]
            stays = jnp.logical_and(at.grp == at.quad // 2, at.quad == k)
            ours = at.quad % 2 == parity

            @pl.when(jnp.logical_and(ours, jnp.logical_not(stays)))
            def _():
                act(functools.partial(send, src, dst, self.down_sems.at[0, k], recv, (at.quad // 2, k, at.exp)))

            @pl.when(jnp.logical_and(ours, stays))
            def _():
                act_local(functools.partial(pltpu.make_async_copy, src, dst, recv))

    def start(self):
        self.over_down(lambda copy: copy().start(), lambda copy: copy().start())
        self.over(lambda copy: copy.start(), lambda copy: copy.start())

    def arrive(self):
        at = self.at
        for rep in range(at.reps):
            for section in self.sections:
                _, dst = self.target(rep // QUAD, rep % QUAD, rep % 2, section)
                arrived(dst, self.sems.at[1, section * at.reps + rep])
        for k, piece in enumerate(self.tiles.rows(self.tile)):
            if piece is None or self.down is None:
                continue

            @pl.when(at.quad == k)
            def _():
                for g in range(at.grps):
                    arrived(self.down_parts.at[g, pl.ds(piece[0], piece[1])], self.down_sems.at[1, g])

    def sent(self):
        self.over(lambda copy: copy.wait_send(), None)
        self.over_down(lambda copy: copy().wait_send(), lambda copy: None)


def forward_kernel(
    grps,
    exps,
    lengths,
    bias_table,
    routes_t,
    tokens,
    cotangent,
    gains,
    router,
    attn_qkv,
    attn_out,
    expert_in,
    expert_out,
    both_w,
    down_w,
    cot_all,
    n_all,
    comb_all,
    qkv_out,
    lse_out,
    mine_out,
    n1_out,
    wqkv_out,
    wout_out,
    h1_out,
    n2_out,
    probs_out,
    in_out,
    down_out,
    in_wide,
    down_wide,
    qkv_t,
    out_w,
    in_low,
    down_slab,
    tok_all,
    wqkv,
    wout,
    n1,
    qkv,
    lse,
    mine,
    ctx,
    bias,
    comb_send,
    nothing,
    tok_sem,
    wq_sem,
    wo_sem,
    wo2_sem,
    weight_sem,
    down_sem,
    ctx_sem,
    cot_sem,
    cot_core_sem,
    n_sem,
    n_core_sem,
    comb_sem,
    store_sem,
    cast_sem,
):
    at = Where(grps, exps)
    reps = at.reps
    rows, width = tokens.shape
    heads = HEADS // exps
    head_dim = width // HEADS
    head_cols = heads * head_dim
    block_cols = min(128, head_cols)
    shard_cols, row_block = qkv_t.shape
    seg = math.gcd(shard_cols, head_cols)
    segs = shard_cols // seg
    tiles = Tiles(down_slab.shape[0], reps)
    plane = at.quad * exps + at.exp
    members = QUAD * exps
    scale = 1.0 / math.sqrt(head_dim)
    SEND, RECV = 0, 1

    wide_copies = [
        pltpu.make_async_copy(expert_in, in_wide, cast_sem.at[0]),
        pltpu.make_async_copy(expert_out, down_wide, cast_sem.at[1]),
    ]
    for copy in wide_copies:
        copy.start()
    qkv_t[...] = attn_qkv[...].T.astype(low)
    out_w[...] = attn_out[...].astype(low)
    greet(at, *everyone(at))

    def exp_peer(k):
        return (at.exp + k) % exps

    group_tokens = Group(at, tokens, tok_all, tok_sem)
    group_tokens.start()
    tok_all[at.exp] = tokens[...]

    def segment(k):
        col = (at.rep * segs + k) * seg
        section = col // width
        within = col - section * width
        owner = within // head_cols
        return owner, section * head_cols + within - owner * head_cols

    def segment_copy(k, shift):
        owner, offset = segment(k)
        src = qkv_t.at[pl.ds(k * seg, seg)]
        dst = wqkv.at[at.exp, pl.ds(pl.multiple_of(offset, seg), seg)]
        target = at.device((at.rep + shift) % reps, owner)
        return owner, src, dst, functools.partial(
            send, src, dst, wq_sem.at[SEND, k * reps + shift], wq_sem.at[RECV, at.exp * 3 * (head_cols // seg) + offset // seg], target
        )

    def over_segments(act, act_local):
        def one(i, _):
            k, shift = i // reps, i % reps
            owner, src, dst, copy = segment_copy(k, shift)
            stays = jnp.logical_and(shift == 0, owner == at.exp)

            @pl.when(jnp.logical_not(stays))
            def _():
                act(copy())

            @pl.when(stays)
            def _():
                act_local(k, src, dst)

            return 0

        lax.fori_loop(0, segs * reps, one, 0)

    def local_segment(k, src, dst):
        _, offset = segment(k)
        pltpu.make_async_copy(src, dst, wq_sem.at[RECV, at.exp * 3 * (head_cols // seg) + offset // seg]).start()

    over_segments(lambda copy: copy.start(), local_segment)

    for k in range(1, reps):
        other = (at.rep + k) % reps
        send(
            out_w, wout.at[at.exp, at.rep], wo_sem.at[SEND, other], wo_sem.at[RECV, at.rep], at.device(other, at.exp)
        ).start()
    wout[at.exp, at.rep] = out_w[...]
    chip_bits = list(range(bits_of(members) - 1))
    cots = Doubling(at, cotangent, cot_all, cot_sem, cot_core_sem, [chip_bits[::-1]] * 3)
    cots.start()

    span = 2 * rows
    bucket = bucket_of(lane_of((8, span)) - rows)
    for h in range(heads):
        line = jnp.zeros((8, span), full)
        for b in range(BUCKETS):
            line = jnp.where(bucket == b, bias_table[at.exp * heads + h, b], line)
        whole = jnp.broadcast_to(line[0:1], (rows, span))
        bias[h] = pltpu.roll(whole, 0, 1, stride=1, stride_axis=0)[:, rows:]

    group_tokens.pass_on()
    group_tokens.arrive()

    def norm_group(s, _):
        x = tok_all[s].astype(full)
        r = lax.rsqrt(jnp.mean(x * x, axis=1, keepdims=True) + eps_norm)
        n1[s] = (x * r * gains[0:1, :]).astype(low)
        return 0

    lax.fori_loop(0, exps, norm_group, 0)

    for copy in wide_copies:
        copy.wait()
    in_low[...] = in_wide[...].astype(low)
    down_slab[...] = down_wide[...].astype(low)
    nothing[...] = jnp.zeros_like(nothing)
    weights = [
        Outward(
            at, tiles, t, in_low, down_slab, both_w.at[t], down_w.at[t], nothing, weight_sem.at[t], down_sem.at[t]
        )
        for t in range(2)
    ]
    weights[0].start()

    def wait_segment(i, _):
        e, j = i // (3 * head_cols // seg), i % (3 * head_cols // seg)
        arrived(wqkv.at[e, pl.ds(pl.multiple_of(j * seg, seg), seg)], wq_sem.at[RECV, i])
        return 0

    lax.fori_loop(0, exps * 3 * head_cols // seg, wait_segment, 0)

    def project(s, _):
        total = jnp.zeros((rows, 3 * head_cols), full)
        for e in range(exps):
            total = total + nt(n1[s, :, e * row_block : (e + 1) * row_block], wqkv[e])
        qkv[s] = total.astype(low)
        return 0

    lax.fori_loop(0, exps, project, 0)

    group_wout = Group(at, wout.at[at.exp], wout, wo2_sem)

    def beside(k):
        if k == 1:
            for j in range(1, reps):
                other = (at.rep + j) % reps
                arrived(wout.at[at.exp, other], wo_sem.at[RECV, other])
            group_wout.start()
        elif k == 2:
            cots.next(0)
        else:
            group_wout.pass_on()

    def attend(i, _):
        s = turn(at.exp, i)
        for k in range(1, exps):

            @pl.when(i == k)
            def _():
                beside(k)

        ok = lane_of((rows, rows)) < lengths[at.base + s]
        lane = lane_of((rows, block_cols))
        sums = jnp.zeros((rows, 128), full)
        for c in range(head_cols // block_cols):
            cols = slice(c * block_cols, (c + 1) * block_cols)
            q = qkv[s, :, cols] * scale
            k = qkv[s, :, head_cols + c * block_cols : head_cols + (c + 1) * block_cols]
            v = qkv[s, :, 2 * head_cols + c * block_cols : 2 * head_cols + (c + 1) * block_cols]
            result = jnp.zeros((rows, block_cols), full)
            for t in range(block_cols // head_dim):
                h = c * (block_cols // head_dim) + t
                here = jnp.logical_and(lane >= t * head_dim, lane < (t + 1) * head_dim)
                scores = nt(jnp.where(here, q, jnp.zeros_like(q)), k) + bias[h]
                scores = jnp.where(ok, scores, -1e30)
                top = jnp.max(scores, axis=1, keepdims=True)
                weights = jnp.exp(scores - top)
                total = jnp.sum(weights, axis=1, keepdims=True)
                weights = (weights * (1.0 / total)).astype(low)
                result = jnp.where(here, jnp.dot(weights, v, preferred_element_type=full), result)
                sums = jnp.where(lane_of((rows, 128)) == h, top + jnp.log(total), sums)
            mine[s, :, cols] = result.astype(low)
        lse[s] = sums

        @pl.when(i < exps - 1)
        def _():
            send(
                mine.at[s], ctx.at[at.exp], ctx_sem.at[SEND, s], ctx_sem.at[RECV, at.exp], at.device(at.rep, s)
            ).start()

        @pl.when(i == exps - 1)
        def _():
            pltpu.make_async_copy(mine.at[s], ctx.at[at.exp], ctx_sem.at[RECV, at.exp]).start()

        return 0

    lax.fori_loop(0, exps, attend, 0)

    cots.next(1)
    group_wout.arrive()
    for e in range(exps):
        arrived(ctx.at[e], ctx_sem.at[RECV, e])

    out_cols = wout.shape[3]
    for r in range(reps):
        cols = slice(r * out_cols, (r + 1) * out_cols)
        total = tokens[:, cols].astype(full)
        for e in range(exps):
            total = total + jnp.dot(ctx[e], wout[e, r], preferred_element_type=full)
        h1_out[:, cols] = total
    h1 = h1_out[...]
    r2 = lax.rsqrt(jnp.mean(h1 * h1, axis=1, keepdims=True) + eps_norm)
    n2 = (h1 * r2 * gains[1:2, :]).astype(low)
    n2_out[...] = n2
    rotated = [chip_bits[c:] + chip_bits[:c] for c in range(3)]
    rows_two = Doubling(at, n2_out, n_all, n_sem, n_core_sem, rotated)
    rows_two.start()
    weights[1].start()

    router_rows = jnp.concatenate([router[...], jnp.zeros((128 - exps, width), full)], axis=0)
    logits = nt(n2.astype(full), router_rows, precision=highest)
    lane = lane_of((rows, 128))
    logits = jnp.where(lane < exps, logits, -1e30)
    probs = jnp.exp(logits - jnp.max(logits, axis=1, keepdims=True))
    probs = probs / jnp.sum(probs, axis=1, keepdims=True)
    probs_out[...] = probs
    picked = jnp.where(routed(routes_t, at.me, rows), probs, 0.0)
    comb = picked / jnp.sum(picked, axis=1, keepdims=True)
    comb = jnp.where(row_of((rows, 1)) < lengths[at.me], comb, 0.0)
    comb_send[...] = comb.T[0 : comb_send.shape[0]]

    def comb_copy(k):
        other = (plane + k) % members
        return send(
            comb_send,
            comb_all.at[plane],
            comb_sem.at[SEND, other],
            comb_sem.at[RECV, plane],
            (at.grp, other // exps, other % exps),
        )

    def start_comb(k, _):
        comb_copy(k).start()
        return 0

    lax.fori_loop(1, members, start_comb, 0)
    pltpu.make_async_copy(comb_send, comb_all.at[plane], comb_sem.at[RECV, plane]).start()
    rows_two.next(0)

    stores = [
        (qkv, qkv_out),
        (lse, lse_out),
        (mine, mine_out),
        (n1, n1_out),
        (wqkv, wqkv_out),
        (wout, wout_out),
        (in_low, in_out),
        (down_slab, down_out),
    ]
    for i, (src, dst) in enumerate(stores):
        pltpu.make_async_copy(src, dst, store_sem.at[i]).start()

    for step in range(1, rows_two.steps):
        rows_two.next(step)
    for step in range(2, cots.steps):
        cots.next(step)

    cots.finish_in()
    rows_two.finish_in()

    def comb_in(k, _):
        arrived(comb_all.at[k], comb_sem.at[RECV, k])
        return 0

    lax.fori_loop(0, members, comb_in, 0)
    for tile in weights:
        tile.arrive()

    for k in range(1, exps):
        peer = exp_peer(k)
        arrived(mine.at[peer], ctx_sem.at[SEND, peer])
    over_segments(lambda copy: copy.wait_send(), lambda k, src, dst: None)
    for k in range(1, reps):
        arrived(out_w, wo_sem.at[SEND, (at.rep + k) % reps])
    group_tokens.sent()
    group_wout.sent()
    cots.finish_out()
    rows_two.finish_out()

    def sent_comb(k, _):
        comb_copy(k).wait_send()
        return 0

    lax.fori_loop(1, members, sent_comb, 0)
    for tile in weights:
        tile.sent()
    for i, (src, dst) in enumerate(stores):
        pltpu.make_async_copy(src, dst, store_sem.at[i]).wait()


def forward_call(
    grps, exps, lengths, bias_table, routes_t, tokens, cotangent, gains, router, attn_qkv, attn_out, expert_in, expert_out
):
    reps = grps * QUAD
    rows, width = tokens.shape
    head_cols = width // exps
    row_block, shard_cols = attn_qkv.shape
    seg = math.gcd(shard_cols, head_cols)
    segs = shard_cols // seg
    units = expert_out.shape[0]
    out_cols = attn_out.shape[1]
    heads = HEADS // exps
    members = QUAD * exps
    tiles = Tiles(units, reps)
    shape = jax.ShapeDtypeStruct
    vmem = pl.BlockSpec(memory_space=pltpu.VMEM)
    smem = pl.BlockSpec(memory_space=pltpu.SMEM)
    hbm = pl.BlockSpec(memory_space=pl.ANY)
    results = [
        (shape((2, width, 2 * tiles.size), low), hbm),
        (shape((2, tiles.size, width), low), hbm),
        (shape((members, rows, width), low), hbm),
        (shape((members, rows, width), low), hbm),
        (shape((members, 8, rows), full), hbm),
        (shape((exps, rows, 3 * head_cols), low), hbm),
        (shape((exps, rows, 128), full), hbm),
        (shape((exps, rows, head_cols), low), hbm),
        (shape((exps, rows, width), low), hbm),
        (shape((exps, 3 * head_cols, row_block), low), hbm),
        (shape((exps, reps, row_block, out_cols), low), hbm),
        (shape((rows, width), full), vmem),
        (shape((rows, width), low), vmem),
        (shape((rows, 128), full), vmem),
        (shape(expert_in.shape, low), hbm),
        (shape(expert_out.shape, low), hbm),
    ]
    dma = pltpu.SemaphoreType.DMA
    chips = members // 2
    return pl.pallas_call(
        functools.partial(forward_kernel, grps, exps),
        out_shape=[r[0] for r in results],
        in_specs=[smem] * 2 + [vmem] * 7 + [hbm] * 2,
        out_specs=[r[1] for r in results],
        scratch_shapes=[
            pltpu.VMEM(expert_in.shape, full),
            pltpu.VMEM(expert_out.shape, full),
            pltpu.VMEM((shard_cols, row_block), low),
            pltpu.VMEM((row_block, out_cols), low),
            pltpu.VMEM(expert_in.shape, low),
            pltpu.VMEM(expert_out.shape, low),
            pltpu.VMEM((exps, rows, width), low),
            pltpu.VMEM((exps, 3 * head_cols, row_block), low),
            pltpu.VMEM((exps, reps, row_block, out_cols), low),
            pltpu.VMEM((exps, rows, width), low),
            pltpu.VMEM((exps, rows, 3 * head_cols), low),
            pltpu.VMEM((exps, rows, 128), full),
            pltpu.VMEM((exps, rows, head_cols), low),
            pltpu.VMEM((exps, rows, head_cols), low),
            pltpu.VMEM((heads, rows, rows), full),
            pltpu.VMEM((8, rows), full),
            pltpu.VMEM((tiles.skip, width), low),
            dma((2, exps)),
            dma((2, max(segs * reps, exps * 3 * head_cols // seg))),
            dma((2, reps)),
            dma((2, exps)),
            dma((2, 2, 2 * reps)),
            dma((2, 2, reps + 1)),
            dma((2, exps)),
            dma((2, 3 * chips)),
            dma((2, 3 * chips + 1)),
            dma((2, 3 * chips)),
            dma((2, 3 * chips + 1)),
            dma((2, members)),
            dma((8,)),
            dma((2,)),
        ],
        compiler_params=pltpu.CompilerParams(
            collective_id=0, has_side_effects=True, vmem_limit_bytes=60 * 1024 * 1024
        ),
        name="forward",
    )(lengths, bias_table, routes_t, tokens, cotangent, gains, router, attn_qkv, attn_out, expert_in, expert_out)


def expert_kernel(
    grps,
    exps,
    cap,
    deal,
    routes_t,
    comb,
    n_all,
    cot_all,
    both_w,
    down_w,
    in_low,
    down_slab,
    h1,
    n_half,
    y_half,
    n_far,
    y_far,
    c_sum,
    both_g,
    down_g,
    in_parts,
    down_parts,
    place,
    marks,
    n_rows,
    g_rows,
    both_v,
    down_v,
    raw_n,
    raw_g,
    y_acc,
    n_acc,
    both_d,
    active,
    both_stage,
    down_stage,
    out_n,
    out_y,
    load_sem,
    raw_sem,
    out_sem,
    in_sem,
    in_down_sem,
    home_sem,
    home_down_sem,
    stage_sem,
    far_sem,
):
    at = Where(grps, exps)
    rows, width = n_all.shape[1:]
    tiles = Tiles(down_slab.shape[0], at.reps)
    size = tiles.size
    slots = exps * cap
    members = QUAD * exps
    loads = [pltpu.make_async_copy(both_w.at[t], both_v.at[t], load_sem.at[0, t]) for t in range(2)] + [
        pltpu.make_async_copy(down_w.at[t], down_v.at[t], load_sem.at[1, t]) for t in range(2)
    ]
    for copy in loads:
        copy.start()

    def raw_copies(q):
        here = pl.ds(pl.multiple_of(q * exps, exps), exps)
        return [
            pltpu.make_async_copy(n_all.at[here], raw_n.at[q % 2], raw_sem.at[0, q % 2]),
            pltpu.make_async_copy(cot_all.at[here], raw_g.at[q % 2], raw_sem.at[1, q % 2]),
        ]

    for copy in raw_copies(0):
        copy.start()

    def partner(k):
        rep = jnp.where(k < at.reps, (at.rep + k) % at.reps, at.rep)
        return at.device(rep, jnp.where(k < at.reps, at.exp, beside))

    beside = at.exp + 1 - 2 * (at.exp % 2)
    greet(at, at.reps, partner)
    last = tiles.count - 1
    incoming = Outward(
        at, tiles, last, in_low, down_slab, both_v.at[last], down_v.at[last], None, in_sem, in_down_sem
    )
    incoming.start()
    home = Homeward(
        at, tiles, 0, both_stage.at[0], down_stage.at[0], in_parts, down_parts, home_sem, home_down_sem, (0,)
    )

    earlier = jnp.where(row_of((rows, rows)) < lane_of((rows, rows)), 1.0, 0.0).astype(low)
    slot = row_of((cap, rows)).astype(full)

    def dispatch(q, _):
        @pl.when(q + 1 < QUAD)
        def _():
            for copy in raw_copies(q + 1):
                copy.start()

        for copy in raw_copies(q):
            copy.wait()
        lines = []
        for j in range(exps):
            seq = at.grp * members + q * exps + j
            pair = routes_t[:, pl.ds(pl.multiple_of(seq * rows, rows), rows)]
            lines.append(jnp.logical_or(pair[0:1] == at.exp, pair[1:2] == at.exp))
        lines = [jnp.where(line, 1.0, 0.0) for line in lines] + [jnp.zeros((8 - exps, rows), full)]
        hot_low = jnp.concatenate(lines, axis=0).astype(low)
        before = dot(hot_low, earlier)
        for j in range(exps):
            s = q * exps + j
            inside = jnp.logical_and(slot == before[j : j + 1, :], hot_low[j : j + 1, :].astype(full) > 0.5)
            here = jnp.where(inside, 1.0, 0.0)
            place[s] = here.astype(low)
            g = raw_g[q % 2, 0]
            for b in range(1, exps):
                g = jnp.where(deal[at.grp * members + s] == at.grp * members + q * exps + b, raw_g[q % 2, b], g)
            where = pl.ds(pl.multiple_of(s * cap, cap), cap)
            n_rows[where] = dot(here.astype(low), raw_n[q % 2, j]).astype(low)
            g_rows[where] = dot(here.astype(low), g).astype(low)
            marks[where, 0:1] = jnp.sum(here * comb[s, pl.ds(at.exp, 1), :], axis=1, keepdims=True)
            marks[where, 1:2] = jnp.zeros((cap, 1), full)
        return 0

    lax.fori_loop(0, QUAD, dispatch, 0)
    for copy in loads:
        copy.wait()
    curve = math.sqrt(2.0 / math.pi)

    core = at.exp % 2

    def half_copies(j):
        return [
            pltpu.make_async_copy(out_n.at[j % 2], n_half.at[j], out_sem.at[0, j % 2]),
            pltpu.make_async_copy(out_y.at[j % 2], y_half.at[j], out_sem.at[1, j % 2]),
        ]

    def far_copies(j):
        device = at.device(at.rep, beside)
        return [
            send(raw.at[j // exps, j % exps], far.at[j], far_sem.at[i, 0, j], far_sem.at[i, 1, j], device)
            for i, (raw, far) in enumerate(((raw_n, n_far), (raw_g, y_far)))
        ]

    def slots_of(s):
        return pl.ds(pl.multiple_of(s * cap, cap), cap)

    def n_rows_of(s):
        where = slots_of(s)
        line = jnp.sum(place[s].astype(full) * marks[where, 1:2], axis=0, keepdims=True)
        c_sum[s] = jnp.broadcast_to(line, (8, rows))
        return tn(place[s], n_acc[where].astype(low)).astype(low)

    def y_rows_of(p):
        first = p // exps * exps
        spot = at.grp * members + p
        here, y = place[first], y_acc[slots_of(first)]
        for c in range(1, exps):
            taken = deal[at.grp * members + first + c] == spot
            here = jnp.where(taken, place[first + c], here)
            y = jnp.where(taken, y_acc[slots_of(first + c)], y)
        return (tn(here, y) + jnp.where(deal[at.me] == spot, h1[...], 0.0)).astype(low)

    def give_back(j, _):
        @pl.when(j >= 2)
        def _():
            for copy in half_copies(j - 2):
                copy.wait()

        out_n[j % 2] = n_rows_of(2 * j + core)
        out_y[j % 2] = y_rows_of(2 * j + core)
        for copy in half_copies(j):
            copy.start()
        raw_n[j // exps, j % exps] = n_rows_of(2 * j + 1 - core)
        raw_g[j // exps, j % exps] = y_rows_of(2 * j + 1 - core)
        for copy in far_copies(j):
            copy.start()
        return 0

    def tile_work(f, _):
        @pl.when(f == last)
        def _():
            incoming.arrive()

        def chunk(c, _):
            here = pl.ds(pl.multiple_of(c * slots, slots), slots)
            share = marks[here, 0:1]
            both = dot(n_rows[here], both_v[f])
            gate_part, up_part = both[:, :size], both[:, size:]
            grad = nt(g_rows[here], down_v[f])
            square = gate_part * gate_part
            bend = jnp.tanh(curve * gate_part * (1.0 + 0.044715 * square))
            half = 0.5 * (1.0 + bend)
            gelu = gate_part * half
            slope = half + (0.5 * curve) * gate_part * (1.0 - bend * bend) * (1.0 + (3 * 0.044715) * square)
            value = gelu * up_part
            marks[here, 1:2] += jnp.sum(value * grad, axis=1, keepdims=True)
            grad = grad * share
            active[here] = (value * share).astype(low)
            both_d[here, :size] = (grad * up_part * slope).astype(low)
            both_d[here, size:] = (grad * gelu).astype(low)
            y = dot(active[here], down_v[f])
            y_acc[here] = jnp.where(f == 0, y, y_acc[here].astype(full) + y).astype(low)
            n_back = nt(both_d[here], both_v[f])
            n_acc[here] = jnp.where(f == 0, n_back, n_acc[here] + n_back)
            return 0

        lax.fori_loop(0, QUAD, chunk, 0)

        @pl.when(f == last)
        def _():
            lax.fori_loop(0, members // 2, give_back, 0)

        def columns(m, _):
            cols = pl.ds(pl.multiple_of(m * (width // 2), width // 2), width // 2)
            both_stage[f, cols] = tn(n_rows[:, cols], both_d[...]).astype(low)
            down_stage[f, :, cols] = tn(active[...], g_rows[:, cols]).astype(low)
            return 0

        lax.fori_loop(0, 2, columns, 0)

        for copy in stage_copies(f):
            copy.start()

        @pl.when(f == 0)
        def _():
            home.start()

        @pl.when(f > 0)
        def _():
            down_copy(f).start()

        return 0

    def stage_copies(f):
        return [pltpu.make_async_copy(both_stage.at[f], both_g.at[f], stage_sem.at[0, f])]

    def down_copy(f):
        return pltpu.make_async_copy(down_stage.at[f], down_g.at[f - 1], stage_sem.at[1, f])

    lax.fori_loop(0, tiles.count, tile_work, 0)

    for j in (members // 2 - 2, members // 2 - 1):
        for copy in half_copies(j):
            copy.wait()
    for f in range(tiles.count):
        for copy in stage_copies(f):
            copy.wait()
        if f:
            down_copy(f).wait()

    def core_in(j, _):
        for copy in far_copies(j):
            copy.wait_send()
        arrived(n_far.at[j], far_sem.at[0, 1, j])
        arrived(y_far.at[j], far_sem.at[1, 1, j])
        return 0

    lax.fori_loop(0, members // 2, core_in, 0)
    home.arrive()
    incoming.sent()
    home.sent()


def expert_call(grps, exps, cap, deal, routes_t, comb_all, n_all, cot_all, both_w, down_w, in_low, down_slab, h1):
    members, rows, width = n_all.shape
    reps = grps * QUAD
    tiles = Tiles(down_slab.shape[0], reps)
    size = tiles.size
    slab, both_hidden = in_low.shape
    units = down_slab.shape[0]
    slots = exps * cap
    shape = jax.ShapeDtypeStruct
    vmem = pl.BlockSpec(memory_space=pltpu.VMEM)
    smem = pl.BlockSpec(memory_space=pltpu.SMEM)
    hbm = pl.BlockSpec(memory_space=pl.ANY)
    results = [
        (shape((members // 2, rows, width), low), hbm),
        (shape((members // 2, rows, width), low), hbm),
        (shape((members // 2, rows, width), low), hbm),
        (shape((members // 2, rows, width), low), hbm),
        (shape((members, 8, rows), full), vmem),
        (shape((tiles.count, width, 2 * size), low), hbm),
        (shape((2, size, width), low), hbm),
        (shape((grps, slab, both_hidden), low), hbm),
        (shape((grps, units, width), low), hbm),
    ]
    dma = pltpu.SemaphoreType.DMA
    return pl.pallas_call(
        functools.partial(expert_kernel, grps, exps, cap),
        out_shape=[r[0] for r in results],
        in_specs=[smem] + [vmem] * 2 + [hbm] * 6 + [vmem],
        out_specs=[r[1] for r in results],
        scratch_shapes=[
            pltpu.VMEM((members, cap, rows), low),
            pltpu.VMEM((QUAD * slots, 128), full),
            pltpu.VMEM((QUAD * slots, width), low),
            pltpu.VMEM((QUAD * slots, width), low),
            pltpu.VMEM((tiles.count, width, 2 * size), low),
            pltpu.VMEM((tiles.count, size, width), low),
            pltpu.VMEM((2, exps, rows, width), low),
            pltpu.VMEM((2, exps, rows, width), low),
            pltpu.VMEM((QUAD * slots, width), low),
            pltpu.VMEM((QUAD * slots, width), full),
            pltpu.VMEM((QUAD * slots, 2 * size), low),
            pltpu.VMEM((QUAD * slots, size), low),
            pltpu.VMEM((tiles.count, width, 2 * size), low),
            pltpu.VMEM((tiles.count, size, width), low),
            pltpu.VMEM((2, rows, width), low),
            pltpu.VMEM((2, rows, width), low),
            dma((2, 2)),
            dma((2, 2)),
            dma((2, 2)),
            dma((2, 2 * reps)),
            dma((2, reps + 1)),
            dma((2, 2 * reps)),
            dma((2, max(QUAD, grps))),
            dma((2, tiles.count)),
            dma((2, 2, members // 2)),
        ],
        compiler_params=pltpu.CompilerParams(
            collective_id=2, has_side_effects=True, vmem_limit_bytes=60 * 1024 * 1024
        ),
        name="experts",
    )(deal, routes_t, comb_all, n_all, cot_all, both_w, down_w, in_low, down_slab, h1)


def adamw_root(weight, moment, second, gradient, step_rate, decay_factor):
    new_moment = beta_one * moment + (1.0 - beta_one) * gradient
    new_second = beta_two * second + (1.0 - beta_two) * gradient * gradient
    root = lax.rsqrt(new_second * (1.0 / (1.0 - beta_two**STEP)))
    step = new_moment * (root * (1.0 - eps_adam * root))
    keep = 1.0 - step_rate * decay_factor
    return (new_moment, new_second, keep * weight - (step_rate / (1.0 - beta_one**STEP)) * step)


def adam_kernel(exps, *refs):
    in_parts, down_parts, qkv_grad, out_grad, small = refs[:5]
    states, news, bias_grad = refs[5:26], refs[26:47], refs[47]
    heads = HEADS // exps
    width = small.shape[1]

    def update(i, grad, rate, decay):
        weight, first, second = [state[...] for state in states[3 * i : 3 * i + 3]]
        values = adamw_root(weight, first, second, grad, rate, decay)
        for new, value in zip(news[3 * i : 3 * i + 3], values, strict=True):
            new[...] = value

    def total(parts):
        result = parts[0].astype(full)
        for k in range(1, parts.shape[0]):
            result = result + parts[k].astype(full)
        return result

    @pl.when(pl.program_id(0) == 0)
    def _():
        update(0, qkv_grad[...], 1.5 / math.sqrt(D), 0.1)
        update(1, out_grad[...], 6.0 / math.sqrt(D), 0.1)
        for e in range(exps):
            for h in range(heads):
                bias_grad[e * heads + h : e * heads + h + 1, :] = small[
                    exps + 3 + e : exps + 4 + e, h * 128 : h * 128 + BUCKETS
                ]
        update(2, bias_grad[...], 0.3, 0.0)
        update(3, small[0:exps, :], 1.0 / math.sqrt(D), 0.1)
        update(4, small[exps : exps + 2, :], 0.5, 0.0)

    update(5, total(in_parts), 1.5 / math.sqrt(D), 0.1)
    update(6, total(down_parts), 1.5 / math.sqrt(FF), 0.1)


def adam_call(exps, in_parts, down_parts, qkv_grad, out_grad, small, states):
    steps = 4

    def whole(array):
        return pl.BlockSpec(array.shape, lambda i: (0,) * array.ndim)

    def columns(array):
        block = array.shape[:-1] + (array.shape[-1] // steps,)
        return pl.BlockSpec(block, lambda i: (0,) * (array.ndim - 1) + (i,))

    specs = [whole(state) for state in states[:15]]
    specs += [columns(state) for state in states[15:18]] + [columns(state) for state in states[18:]]
    return pl.pallas_call(
        functools.partial(adam_kernel, exps),
        grid=(steps,),
        in_specs=[columns(in_parts), columns(down_parts), whole(qkv_grad), whole(out_grad), whole(small)] + specs,
        out_specs=specs,
        out_shape=[jax.ShapeDtypeStruct(state.shape, full) for state in states],
        scratch_shapes=[pltpu.VMEM((HEADS, BUCKETS), full)],
        compiler_params=pltpu.CompilerParams(vmem_limit_bytes=60 * 1024 * 1024),
        name="adam",
    )(in_parts, down_parts, qkv_grad, out_grad, small, *states)


class Halving:
    def __init__(self, at, half, far, kept, bufs, sems, load_sem, orders):
        self.at, self.half, self.far, self.kept, self.bufs = at, half, far, kept, bufs
        self.sems, self.load_sem = sems, load_sem
        self.plane = at.quad * at.exps + at.exp
        self.places = bits_of(QUAD * at.exps)
        self.chip_bits = list(range(self.places - 1))
        self.parts = column_parts(half.shape[2])
        self.orders = orders

    def device(self, bit):
        other = flipped(self.plane, bit)
        return (self.at.grp, other // self.at.exps, other % self.at.exps)

    def loads(self, j):
        return [
            pltpu.make_async_copy(self.far.at[j], self.bufs[0].at[j], self.load_sem.at[0, j]),
            pltpu.make_async_copy(self.half.at[j], self.kept.at[j], self.load_sem.at[1, j]),
        ]

    def start_first(self):
        def one(j, _):
            for copy in self.loads(j):
                copy.start()
            return 0

        lax.fori_loop(0, self.half.shape[0], one, 0)

    def add_first(self):
        def one(j, _):
            for copy in self.loads(j):
                copy.wait()
            self.bufs[0][j] = self.bufs[0][j] + self.kept[j]
            return 0

        lax.fori_loop(0, self.half.shape[0], one, 0)

    def hop(self, step, part):
        order = self.orders[part]
        bit = order[step]
        left = [b for b in self.chip_bits if b not in order[:step]]
        pos = left.index(bit)
        half = 1 << (len(left) - 1)
        mine = (self.plane // (1 << (bit + 1))) % 2
        device = self.device(bit + 1)
        begin, size = self.parts[part]
        cols = pl.ds(begin, size)
        base = self.base(step, part)

        def index(j, value):
            return (j >> pos) * (1 << (pos + 1)) + value * (1 << pos) + j % (1 << pos)

        pairs = []
        for j in range(half):
            copy = functools.partial(
                send,
                self.bufs[step].at[index(j, 1 - mine), :, cols],
                self.bufs[step + 1].at[j, :, cols],
                self.sems.at[0, base + j],
                self.sems.at[1, base + j],
                device,
            )
            pairs.append((copy, index(j, mine), j))
        return pairs, begin, size, base

    def base(self, step, part):
        n = len(self.chip_bits)
        return part * (1 << n) + sum(1 << (n - 1 - s) for s in range(step))

    def start(self, step, part=None):
        for p in range(3) if part is None else [part]:
            for copy, _, _ in self.hop(step, p)[0]:
                copy().start()

    def add(self, step, part):
        pairs, begin, size, base = self.hop(step, part)
        cols = pl.ds(begin, size)
        here, there = self.bufs[step], self.bufs[step + 1]
        for _, keep, j in pairs:
            arrived(there.at[j, :, cols], self.sems.at[1, base + j])
            there[j, :, begin : begin + size] = (
                there[j, :, begin : begin + size] + here[keep, :, begin : begin + size]
            )

    def next(self, step):
        for p in range(3):
            self.add(step, p)
            if step + 1 < len(self.chip_bits):
                self.start(step + 1, p)

    def result(self):
        return self.bufs[len(self.chip_bits)]

    def finish(self):
        for step in range(len(self.chip_bits)):
            for p in range(3):
                for copy, _, _ in self.hop(step, p)[0]:
                    copy().wait_send()


def backward_kernel(
    grps,
    exps,
    lengths,
    deal,
    bias_table,
    n_half,
    y_half,
    n_far,
    y_far,
    c_parts,
    both_g,
    down_g,
    in_before,
    down_before,
    n1_in,
    cot_all,
    routes_t,
    tokens,
    n2_in,
    probs_in,
    h1_from,
    qkv_from,
    lse_from,
    mine_from,
    wqkv_from,
    wout_from,
    gains,
    router_t,
    *rest,
):
    token_grad, block_out, in_parts, down_parts, qkv_grad, out_grad, small_out = rest[:7]
    scratch = rest[7:]
    (
    h1_in,
    qkv,
    lse,
    mine,
    wqkv,
    wout,
    kept,
    n_bufs,
    y_bufs,
    c_in,
    dh1,
    dz_send,
    dz_all,
    do_send,
    do_in,
    bias,
    bias_sum,
    dqkv,
    dqkv_t,
    dn1_send,
    dn1_in,
    wq_send,
    og_send,
    mids,
    far_send,
    far_in,
    small_send,
    small_exp,
    small_sum,
    small_rep,
    n_sem,
    y_sem,
    load_sem,
    c_sem,
    weight_sem,
    down_sem,
    dz_sem,
    do_sem,
    dn1_sem,
    wq_sem,
    og_sem,
    mid_sem,
    far_sem,
    small_sem,
    small2_sem,
    n1_sem,
    operand_sem,
    ) = scratch
    at = Where(grps, exps)
    reps = at.reps
    rows, width = tokens.shape
    heads = HEADS // exps
    head_dim = width // HEADS
    head_cols = heads * head_dim
    block_cols = min(128, head_cols)
    row_block = wqkv.shape[2]
    out_cols = wout.shape[3]
    tiles = Tiles(down_parts.shape[1], reps)
    scale = 1.0 / math.sqrt(head_dim)
    SEND, RECV = 0, 1
    plane = at.quad * exps + at.exp
    members = QUAD * exps

    def exp_peer(k):
        return (at.exp + k) % exps

    router = router_t[...]
    n1 = kept.at[0:exps]
    group = pl.ds(pl.multiple_of(at.quad * exps, exps), exps)
    cot_copy = pltpu.make_async_copy(cot_all.at[group], dn1_send, n1_sem.at[1])
    cot_copy.start()
    loads = [
        pltpu.make_async_copy(src, dst, operand_sem.at[i])
        for i, (src, dst) in enumerate(
            ((h1_from, h1_in), (wout_from, wout), (qkv_from, qkv), (lse_from, lse), (mine_from, mine), (wqkv_from, wqkv))
        )
    ]
    dn = Halving(at, n_half, n_far, kept, n_bufs, n_sem, load_sem.at[0], [[0, 1, 2], [1, 2, 0], [2, 0, 1]])
    ys = Halving(at, y_half, y_far, kept, y_bufs, y_sem, load_sem.at[1], [[0, 1, 2], [0, 1, 2], [1, 0, 2]])
    dn.start_first()
    for copy in loads:
        copy.start()

    def partner(k):
        other = (plane + k) % members
        rest = k - members
        grp = jnp.where(k < members, at.grp, (at.grp + 1 + rest // QUAD) % grps)
        quad = jnp.where(k < members, other // exps, rest % QUAD)
        return grp, quad, jnp.where(k < members, other % exps, at.exp)

    greet(at, members - 1 + QUAD * (grps - 1), partner)

    homes = [
        Homeward(
            at,
            tiles,
            t,
            both_g.at[t],
            down_g.at[t - 1] if t else None,
            in_parts,
            down_parts,
            weight_sem.at[t],
            down_sem.at[t],
            (0, 1) if t else (1,),
        )
        for t in range(tiles.count)
    ]
    dn.add_first()
    dn.start(0)
    ys.start_first()
    homes[0].start()
    n1_copy = pltpu.make_async_copy(n1_in, n1, n1_sem.at[0])

    def c_copy(k):
        other = (plane + k) % members
        return other, send(
            c_parts.at[other],
            c_in.at[plane],
            c_sem.at[SEND, other],
            c_sem.at[RECV, plane],
            (at.grp, other // exps, other % exps),
        )

    def start_c(k, _):
        c_copy(k)[1].start()
        return 0

    lax.fori_loop(1, members, start_c, 0)
    pltpu.make_async_copy(c_parts.at[plane], c_in.at[plane], c_sem.at[RECV, plane]).start()

    span = 2 * rows
    bucket = bucket_of(lane_of((8, span)) - rows)
    for h in range(heads):
        line = jnp.zeros((8, span), full)
        for b in range(BUCKETS):
            line = jnp.where(bucket == b, bias_table[at.exp * heads + h, b], line)
        whole = jnp.broadcast_to(line[0:1], (rows, span))
        bias[h] = pltpu.roll(whole, 0, 1, stride=1, stride_axis=0)[:, rows:]


    def wait_c(k, _):
        arrived(c_in.at[k], c_sem.at[RECV, k])
        return 0

    lax.fori_loop(0, members, wait_c, 0)
    lane = lane_of((rows, 128))
    comb_rows = []
    for e in range(exps):
        total = c_in[e]
        for q in range(1, QUAD):
            total = total + c_in[q * exps + e]
        comb_rows.append(total[0:1, :])
    comb_rows.append(jnp.zeros((128 - exps, rows), full))
    comb_grad = jnp.concatenate(comb_rows, axis=0).T
    valid = row_of((rows, 1)) < lengths[at.me]
    probs = probs_in[...]
    hot = routed(routes_t, at.me, rows)
    picked = jnp.where(hot, probs, 0.0)
    total = jnp.sum(picked, axis=1, keepdims=True)
    gate = picked / total
    gate_grad_rows = jnp.where(valid, comb_grad, 0.0)
    spread_grad = jnp.sum(gate_grad_rows * gate, axis=1, keepdims=True)
    probs_grad = jnp.where(hot, (gate_grad_rows - spread_grad) / total, 0.0)
    logit_grad = probs * (probs_grad - jnp.sum(probs_grad * probs, axis=1, keepdims=True))
    n2 = n2_in[...].astype(full)
    router_rows = lax.dot_general(
        logit_grad, n2, (((0,), (0,)), ((), ())), preferred_element_type=full, precision=highest
    )
    small_rows = small_send.shape[0]
    small_send[...] = jnp.zeros_like(small_send)
    small_send[0:exps, :] = router_rows[0:exps, :]
    router_back = jnp.dot(
        logit_grad, jnp.concatenate([router, jnp.zeros((128 - exps, width), full)], axis=0),
        precision=highest, preferred_element_type=full,
    )
    for copy in loads:
        copy.wait()
    h1 = h1_in[...]
    r2 = lax.rsqrt(jnp.mean(h1 * h1, axis=1, keepdims=True) + eps_norm)

    dn.next(0)
    ys.add_first()
    n1_copy.start()
    dn.next(1)
    homes[1].start()
    steps = len(dn.chip_bits)
    for step in range(2, steps):
        dn.next(step)

    n2_grad = router_back + dn.result()[0].astype(full)
    scaled = n2_grad * gains[1:2, :]
    cot_copy.wait()
    dealt = deal[at.me] - at.base
    g = dn1_send[0]
    for e in range(1, exps):
        g = jnp.where(dealt == e, dn1_send[e], g)
    hidden_grad = (
        jnp.where(valid, g.astype(full), 0.0)
        + r2 * scaled
        - h1 * (r2 * r2 * r2) * jnp.mean(scaled * h1, axis=1, keepdims=True)
    )
    dh1[...] = hidden_grad
    small_send[exps + 1 : exps + 2, :] = jnp.sum(n2_grad * h1 * r2, axis=0, keepdims=True)
    branch = hidden_grad.astype(low)
    dz_send[...] = branch
    for e in range(exps):
        total = jnp.zeros((rows, row_block), full)
        for r in range(reps):
            total = total + nt(branch[:, r * out_cols : (r + 1) * out_cols], wout[e, r])
        do_send[e] = total.astype(low)

    def do_copies():
        return [
            send(
                do_send.at[exp_peer(k)],
                do_in.at[at.exp],
                do_sem.at[SEND, exp_peer(k)],
                do_sem.at[RECV, at.exp],
                at.device(at.rep, exp_peer(k)),
            )
            for k in range(1, exps)
        ]

    for copy in do_copies():
        copy.start()
    pltpu.make_async_copy(do_send.at[at.exp], do_in.at[at.exp], do_sem.at[RECV, at.exp]).start()

    group_dz = Group(at, dz_send, dz_all, dz_sem)
    group_dz.start()
    dz_all[at.exp] = branch
    ys.start(0)
    homes[2].start()

    bias_sum[...] = jnp.zeros_like(bias_sum)

    def dn1_copies():
        beside, across = turn(at.exp, 2), turn(at.exp, 1)
        return [
            functools.partial(
                send, dn1_send.at[k], dn1_in.at[j], dn1_sem.at[SEND, j], dn1_sem.at[RECV, j], at.device(at.rep, to)
            )
            for k, j, to in ((turn(at.exp, 0), 2, beside), (across, 0, across), (beside, 1, beside))
        ]

    def attend_back(i, _):
        s = turn(at.exp, i)
        @pl.when(i == 1)
        def _():
            group_dz.pass_on()

        arrived(do_in.at[s], do_sem.at[RECV, s])
        ok = lane_of((rows, rows)) < lengths[at.base + s]
        block_lane = lane_of((rows, block_cols))
        for c in range(head_cols // block_cols):
            cols = slice(c * block_cols, (c + 1) * block_cols)
            k_cols = slice(head_cols + c * block_cols, head_cols + (c + 1) * block_cols)
            v_cols = slice(2 * head_cols + c * block_cols, 2 * head_cols + (c + 1) * block_cols)
            q = qkv[s, :, cols] * scale
            k = qkv[s, :, k_cols]
            v = qkv[s, :, v_cols]
            do = do_in[s, :, cols]
            dq = jnp.zeros((rows, block_cols), full)
            dk = jnp.zeros((rows, block_cols), full)
            dv = jnp.zeros((rows, block_cols), full)
            for t in range(block_cols // head_dim):
                h = c * (block_cols // head_dim) + t
                here = jnp.logical_and(block_lane >= t * head_dim, block_lane < (t + 1) * head_dim)
                zero = jnp.zeros_like(q)
                q_h = jnp.where(here, q, zero)
                do_h = jnp.where(here, do, zero)
                scores = nt(q_h, k) + bias[h]
                p = jnp.where(ok, jnp.exp(scores - lse[s, :, h : h + 1]), 0.0)
                dp = nt(do_h, v)
                delta = jnp.sum(dp * p, axis=1, keepdims=True)
                ds = (p * (dp - delta)).astype(low)
                bias_sum[h] += ds.astype(full)
                dv = jnp.where(here, tn(p.astype(low), do), dv)
                dq = jnp.where(here, jnp.dot(ds, k, preferred_element_type=full), dq)
                dk = jnp.where(here, tn(ds, q), dk)
            dqkv[:, cols] = (dq * scale).astype(low)
            dqkv[:, k_cols] = dk.astype(low)
            dqkv[:, v_cols] = dv.astype(low)
        dqkv_t[:, pl.ds(pl.multiple_of(s * rows, rows), rows)] = dqkv[...].T
        for e in range(exps):
            dn1_send[s, :, e * row_block : (e + 1) * row_block] = jnp.dot(
                dqkv[...], wqkv[e], preferred_element_type=full
            ).astype(low)

        @pl.when(i == 0)
        def _():
            dn1_copies()[0]().start()

        @pl.when(i == 1)
        def _():
            arrived(dn1_in.at[2], dn1_sem.at[RECV, 2])
            dn1_send[s] = (dn1_send[s].astype(full) + dn1_in[2].astype(full)).astype(low)
            dn1_copies()[1]().start()

        @pl.when(i == 2)
        def _():
            dn1_copies()[2]().start()

        return 0

    lax.fori_loop(0, exps, attend_back, 0)

    n1_copy.wait()
    seg = wq_send.shape[2]
    parts = wq_send.shape[1]
    segs = mids.shape[1] - 1
    for e in range(exps):
        part = kept[0:exps, :, e * row_block : (e + 1) * row_block].reshape(exps * rows, row_block)
        total = dot(dqkv_t[...], part)
        for j in range(parts):
            wq_send[e, j] = total[j * seg : (j + 1) * seg].astype(low)

    def owner(j):
        section, within = j // (head_cols // seg), j % (head_cols // seg)
        col = section * width + at.exp * head_cols + within * seg
        block = col // seg
        return block // segs, block % segs

    def mid_place(grp, k, quad):
        return (grp * (segs + 1) + k) * QUAD + quad

    def mid_copy(src, send_sem, rep, k, e):
        dst = mids.at[rep // QUAD, k, at.quad]
        recv = mid_sem.at[mid_place(rep // QUAD, k, at.quad)]
        stays = jnp.logical_and(rep % QUAD == at.quad, e == at.exp)
        return (
            stays,
            functools.partial(send, src, dst, send_sem, recv, (at.grp, rep % QUAD, e)),
            functools.partial(pltpu.make_async_copy, src, dst, recv),
        )

    def wq_copy(i):
        e, j = i // parts, i % parts
        rep, k = owner(j)
        return mid_copy(wq_send.at[e, j], wq_sem.at[i], rep, k, e)

    def og_copy(r):
        return mid_copy(og_send.at[r], og_sem.at[r], r, segs, at.exp)

    def go(copies, act, act_local):
        stays, away, local = copies

        @pl.when(jnp.logical_not(stays))
        def _():
            act(away)

        if act_local:

            @pl.when(stays)
            def _():
                act_local(local)

    def over(count, copies, act, act_local):
        def one(i, _):
            go(copies(i), act, act_local)
            return 0

        lax.fori_loop(0, count, one, 0)

    over(exps * parts, wq_copy, lambda copy: copy().start(), lambda copy: copy().start())
    group_dz.arrive()
    grad = tn(mine[...].reshape(exps * rows, head_cols), dz_all[...].reshape(exps * rows, width))
    for r in range(reps):
        og_send[r] = grad[:, r * out_cols : (r + 1) * out_cols].T.astype(low)
    over(reps, og_copy, lambda copy: copy().start(), lambda copy: copy().start())

    n1_grad = dn1_send[at.exp].astype(full)
    for j in range(2):
        arrived(dn1_in.at[j], dn1_sem.at[RECV, j])
        n1_grad = n1_grad + dn1_in[j].astype(full)
    x = tokens[...].astype(full)
    r1 = lax.rsqrt(jnp.mean(x * x, axis=1, keepdims=True) + eps_norm)
    scaled = n1_grad * gains[0:1, :]
    token_grad[...] = (
        dh1[...] + r1 * scaled - x * (r1 * r1 * r1) * jnp.mean(scaled * x, axis=1, keepdims=True)
    )
    small_send[exps : exps + 1, :] = jnp.sum(n1_grad * x * r1, axis=0, keepdims=True)

    line_lane = lane_of((8, 128))
    line_row = row_of((8, 128))
    bias_line = jnp.zeros((8, 128), full)
    flip = jnp.where(row_of((rows, rows)) + lane_of((rows, rows)) == rows - 1, 1.0, 0.0).astype(low)
    turned_bucket = bucket_of(rows - 1 - lane_of((8, span)))
    for h in range(heads):
        high = bias_sum[h].astype(low)
        rest = (bias_sum[h] - high.astype(full)).astype(low)
        flipped = dot(high, flip) + dot(rest, flip)
        square = jnp.concatenate([flipped, jnp.zeros((rows, rows), full)], axis=1)
        turned = pltpu.roll(square, 0, 1, stride=1, stride_axis=0)
        sums = jnp.broadcast_to(jnp.sum(turned, axis=0, keepdims=True), (8, span))
        for b in range(BUCKETS):
            value = jnp.sum(jnp.where(turned_bucket == b, sums, 0.0), axis=1, keepdims=True)
            bias_line = jnp.where(jnp.logical_and(line_row == h, line_lane == b), value, bias_line)
    for h in range(heads):
        small_send[exps + 2 : exps + 3, h * 128 : (h + 1) * 128] = bias_line[h : h + 1, :]

    def small_copies():
        return [
            send(
                small_send,
                small_exp.at[at.exp],
                small_sem.at[SEND, exp_peer(k)],
                small_sem.at[RECV, at.exp],
                at.device(at.rep, exp_peer(k)),
            )
            for k in range(1, exps)
        ]

    for copy in small_copies():
        copy.start()
    small_exp[at.exp] = small_send[...]
    ys.next(0)

    def mid_sum(grp, k):
        for q in range(QUAD):
            arrived(mids.at[grp, k, q], mid_sem.at[mid_place(grp, k, q)])
        total = mids[grp, k, 0].astype(full)
        for q in range(1, QUAD):
            total = total + mids[grp, k, q].astype(full)
        return total

    far = 1 - at.grp
    for k in range(segs + 1):
        far_send[k] = mid_sum(far, k).astype(low)

    def far_copy():
        return send(far_send, far_in, far_sem.at[SEND], far_sem.at[RECV], (far, at.quad, at.exp))

    far_copy().start()
    ys.next(1)
    for k in range(1, exps):
        arrived(small_exp.at[exp_peer(k)], small_sem.at[RECV, exp_peer(k)])
    total = small_exp[0]
    for e in range(1, exps):
        total = total + small_exp[e]
    small_sum[0] = total
    for e in range(exps):
        small_sum[0, exps + 3 + e : exps + 4 + e, :] = small_exp[e, exps + 2 : exps + 3, :]

    def small2_copies():
        return [
            send(
                small_sum.at[0],
                small_rep.at[at.rep],
                small2_sem.at[SEND, (at.rep + k) % reps],
                small2_sem.at[RECV, at.rep],
                at.device((at.rep + k) % reps, at.exp),
            )
            for k in range(1, reps)
        ]

    for copy in small2_copies():
        copy.start()
    small_rep[at.rep] = small_sum[0]
    for step in range(2, steps):
        ys.next(step)
    length = lengths[at.base]
    for e in range(1, exps):
        length = jnp.where(deal[at.base + e] == at.me, lengths[at.base + e], length)
    block = ys.result()[0]
    block_out[...] = jnp.where(row_of((rows, 1)) < length, block, jnp.zeros_like(block))
    for k in range(1, reps):
        arrived(small_rep.at[(at.rep + k) % reps], small2_sem.at[RECV, (at.rep + k) % reps])
    total = small_rep[0]
    for r in range(1, reps):
        total = total + small_rep[r]
    small_out[...] = total

    near = [mid_sum(at.grp, k) for k in range(segs + 1)]
    arrived(far_in, far_sem.at[RECV])
    grads = [(near[k] + far_in[k].astype(full)).T for k in range(segs + 1)]
    qkv_grad[...] = jnp.concatenate(grads[:segs], axis=1)
    out_grad[...] = grads[segs]
    for home in homes:
        home.arrive()

    def sent_c(k, _):
        c_copy(k)[1].wait_send()
        return 0

    lax.fori_loop(1, members, sent_c, 0)
    dn.finish()
    ys.finish()

    for home in homes:
        home.sent()

    over(exps * parts, wq_copy, lambda copy: copy().wait_send(), None)
    over(reps, og_copy, lambda copy: copy().wait_send(), None)
    far_copy().wait_send()
    for copies in (do_copies(), small_copies(), small2_copies()):
        for copy in copies:
            copy.wait_send()
    for copy in dn1_copies():
        copy().wait_send()
    group_dz.sent()


def routed(routes_t, seq, rows):
    pair = routes_t[:, pl.ds(pl.multiple_of(seq * rows, rows), rows)].astype(full)
    cols = jnp.concatenate([pair, jnp.zeros((126, rows), full)], axis=0).T
    lane = lane_of((rows, 128)).astype(full)
    return jnp.logical_or(lane == cols[:, 0:1], lane == cols[:, 1:2])


def backward_call(
    grps, exps, lengths, deal, bias_table, n_half, y_half, n_far, y_far, c_parts, both_g, down_g, in_before, down_before, n1,
    cot_all, routes_t, tokens, n2, probs, h1, qkv, lse, mine, wqkv, wout, gains, router
):
    reps = grps * QUAD
    rows, width = tokens.shape
    heads = HEADS // exps
    head_cols = width // exps
    row_block = wqkv.shape[2]
    out_cols = wout.shape[3]
    shard_cols = 3 * width // reps
    seg = math.gcd(shard_cols, head_cols)
    segs = shard_cols // seg
    parts = 3 * head_cols // seg
    members = QUAD * exps
    chip_bits = bits_of(members) - 1
    small_rows = -(-(2 * exps + 3) // 8) * 8
    shape = jax.ShapeDtypeStruct
    vmem = pl.BlockSpec(memory_space=pltpu.VMEM)
    smem = pl.BlockSpec(memory_space=pltpu.SMEM)
    hbm = pl.BlockSpec(memory_space=pl.ANY)
    results = [
        (shape((rows, width), full), vmem),
        (shape((rows, width), low), vmem),
        (shape(in_before.shape, low), hbm),
        (shape(down_before.shape, low), hbm),
        (shape((row_block, shard_cols), full), vmem),
        (shape((row_block, out_cols), full), vmem),
        (shape((small_rows, width), full), vmem),
    ]
    dma = pltpu.SemaphoreType.DMA
    bufs = [pltpu.VMEM((1 << (chip_bits - s), rows, width), low) for s in range(chip_bits + 1)]
    return pl.pallas_call(
        functools.partial(backward_kernel, grps, exps),
        out_shape=[r[0] for r in results],
        in_specs=[smem] * 3 + [hbm] * 11 + [vmem] * 4 + [hbm] * 6 + [vmem] * 2,
        out_specs=[r[1] for r in results],
        scratch_shapes=[
            pltpu.VMEM(h1.shape, full),
            pltpu.VMEM(qkv.shape, low),
            pltpu.VMEM(lse.shape, full),
            pltpu.VMEM(mine.shape, low),
            pltpu.VMEM(wqkv.shape, low),
            pltpu.VMEM(wout.shape, low),
            pltpu.VMEM((members // 2, rows, width), low),
            list(bufs),
            list(bufs),
            pltpu.VMEM((members, 8, rows), full),
            pltpu.VMEM((rows, width), full),
            pltpu.VMEM((rows, width), low),
            pltpu.VMEM((exps, rows, width), low),
            pltpu.VMEM((exps, rows, head_cols), low),
            pltpu.VMEM((exps, rows, head_cols), low),
            pltpu.VMEM((heads, rows, rows), full),
            pltpu.VMEM((heads, rows, rows), full),
            pltpu.VMEM((rows, 3 * head_cols), low),
            pltpu.VMEM((3 * head_cols, exps * rows), low),
            pltpu.VMEM((exps, rows, width), low),
            pltpu.VMEM((3, rows, width), low),
            pltpu.VMEM((exps, parts, seg, row_block), low),
            pltpu.VMEM((reps, seg, row_block), low),
            pltpu.VMEM((grps, segs + 1, QUAD, seg, row_block), low),
            pltpu.VMEM((segs + 1, seg, row_block), low),
            pltpu.VMEM((segs + 1, seg, row_block), low),
            pltpu.VMEM((small_rows, width), full),
            pltpu.VMEM((exps, small_rows, width), full),
            pltpu.VMEM((1, small_rows, width), full),
            pltpu.VMEM((reps, small_rows, width), full),
            dma((2, 3 << chip_bits)),
            dma((2, 3 << chip_bits)),
            dma((2, 2, members // 2)),
            dma((2, members)),
            dma((3, 2, 2 * reps)),
            dma((3, 2, max(QUAD, grps))),
            dma((2, exps)),
            dma((2, exps)),
            dma((2, exps)),
            dma((exps * parts,)),
            dma((reps,)),
            dma((grps * (segs + 1) * QUAD,)),
            dma((2,)),
            dma((2, exps)),
            dma((2, reps)),
            dma((2,)),
            dma((6,)),
        ],
        compiler_params=pltpu.CompilerParams(
            collective_id=1, has_side_effects=True, vmem_limit_bytes=60 * 1024 * 1024
        ),
        input_output_aliases={10: 2, 11: 3},
        name="backward",
    )(
        lengths, deal, bias_table, n_half, y_half, n_far, y_far, c_parts, both_g, down_g, in_before, down_before, n1, cot_all,
        routes_t, tokens, n2, probs, h1, qkv, lse, mine, wqkv, wout, gains, router
    )


def per_device(
    tokens,
    cotangent,
    seq_lengths,
    deal,
    routes,
    attn_qkv,
    qkv_first,
    qkv_second,
    attn_out,
    out_first,
    out_second,
    rel_bias,
    bias_first,
    bias_second,
    router,
    router_first,
    router_second,
    norm_gains,
    gains_first,
    gains_second,
    expert_in,
    in_first,
    in_second,
    expert_out,
    down_first,
    down_second,
):
    rows, width = tokens.shape
    experts = router.shape[1]
    capacity = (10 * rows + 4 * experts - 1) // (4 * experts)
    exps = lax.axis_size("exp")
    grps = lax.axis_size("grp")
    routes_t = routes.T
    bias_table = rel_bias.T
    (
        both_w, down_w, cot_all, n_all, comb_all, qkv, lse, context_mine, normed_group, wqkv, wout, hidden_one,
        normed_two, router_probs, in_low, down_low,
    ) = forward_call(
        grps, exps, seq_lengths, bias_table, routes_t, tokens, cotangent, norm_gains.T, router.T,
        attn_qkv, attn_out, expert_in[0], expert_out[0],
    )
    n_half, y_half, n_far, y_far, c_parts, both_g, down_g, in_before, down_before = expert_call(
        grps, exps, capacity, deal, routes_t, comb_all, n_all, cot_all, both_w, down_w, in_low, down_low,
        hidden_one,
    )
    token_grad, block_out, in_parts, down_parts, qkv_grad, out_grad, small = backward_call(
        grps, exps, seq_lengths, deal, bias_table, n_half, y_half, n_far, y_far, c_parts, both_g, down_g,
        in_before, down_before, normed_group, cot_all, routes_t, tokens, normed_two, router_probs, hidden_one, qkv, lse, context_mine, wqkv,
        wout, norm_gains.T, router.T,
    )
    states = [
        attn_qkv, qkv_first, qkv_second, attn_out, out_first, out_second, bias_table, bias_first.T, bias_second.T,
        router.T, router_first.T, router_second.T, norm_gains.T, gains_first.T, gains_second.T,
        expert_in[0], in_first[0], in_second[0], expert_out[0], down_first[0], down_second[0],
    ]
    new = list(adam_call(exps, in_parts, down_parts, qkv_grad, out_grad, small, states))
    new = new[:6] + [array.T for array in new[6:15]] + [array[None] for array in new[15:]]
    return (block_out, token_grad, *new)


def bucket_onehot(length):
    places = jnp.arange(length, dtype=jnp.int32)
    offset = places[None, :] - places[:, None]
    distance = jnp.abs(offset)
    bucket = 16 * (offset > 0).astype(jnp.int32)
    for threshold in thresholds:
        bucket = bucket + (distance >= threshold).astype(jnp.int32)
    return (bucket[:, :, None] == jnp.arange(BUCKETS, dtype=jnp.int32)[None, None, :]).astype(full)


def swap(pieces, axes):
    return lax.all_to_all(pieces, axes, split_axis=0, concat_axis=0, tiled=True)


def spread(block, axes):
    members = lax.axis_size(axes)
    return swap(jnp.broadcast_to(block[None], (members,) + block.shape), axes)


def plain_device(
    tokens,
    cotangent,
    seq_lengths,
    deal,
    routes,
    attn_qkv,
    qkv_first,
    qkv_second,
    attn_out,
    out_first,
    out_second,
    rel_bias,
    bias_first,
    bias_second,
    router,
    router_first,
    router_second,
    norm_gains,
    gains_first,
    gains_second,
    expert_in,
    in_first,
    in_second,
    expert_out,
    down_first,
    down_second,
):
    rows, width = tokens.shape
    head_dim = width // HEADS
    score_scale = 1.0 / math.sqrt(head_dim)
    experts = router.shape[1]
    capacity = (10 * rows + 4 * experts - 1) // (4 * experts)
    exps = lax.axis_size("exp")
    grps = lax.axis_size("grp")
    reps = grps * QUAD
    heads = HEADS // exps
    head_cols = heads * head_dim
    place = lax.axis_index("exp")
    base = lax.axis_index(REP) * exps
    me = base + place
    slab = expert_in.shape[1]
    units = expert_out.shape[1]
    quarter = grps * units

    row_block = attn_qkv.shape[0]
    qkv_rows = lax.all_gather(attn_qkv.astype(low), REP, axis=1, tiled=True)
    out_rows = lax.all_gather(attn_out.astype(low), REP, axis=1, tiled=True)
    qkv_pieces = jnp.transpose(
        qkv_rows.reshape(row_block, 3, exps, head_cols), (2, 0, 1, 3)
    ).reshape(exps, row_block, 3 * head_cols)
    qkv_mine = swap(qkv_pieces, "exp").reshape(width, 3 * head_cols)
    full_out = spread(out_rows, "exp").reshape(width, width)

    group_tokens = spread(tokens, "exp")
    group_cotangent = spread(cotangent, "exp")
    my_cotangent = lax.dynamic_index_in_dim(group_cotangent, deal[me] - base, 0, keepdims=False)

    my_routes = lax.dynamic_slice_in_dim(routes, me * rows, rows, 0)
    places = jnp.arange(rows, dtype=jnp.int32)
    valid_rows = (places < seq_lengths[me]).astype(full)
    group_lengths = lax.dynamic_slice_in_dim(seq_lengths, base, exps, 0)
    key_ok = places[None, :] < group_lengths[:, None]
    gain_one = norm_gains[:, 0]
    gain_two = norm_gains[:, 1]

    chosen = (my_routes[:, :, None] == jnp.arange(experts, dtype=jnp.int32)[None, None, :]).astype(full)
    flat_routes = my_routes.reshape(-1)
    route_hot = (flat_routes[:, None] == jnp.arange(experts, dtype=jnp.int32)[None, :]).astype(jnp.int32)
    before = jnp.cumsum(route_hot, axis=0) - route_hot
    slot_index = jnp.sum(before * route_hot, axis=-1)
    target = (flat_routes * capacity + slot_index).reshape(rows, 2)
    slots = experts * capacity
    slot_ids = jnp.arange(slots, dtype=jnp.int32)
    place_first = slot_ids[:, None] == target[None, :, 0]
    place_second = slot_ids[:, None] == target[None, :, 1]
    place_any = jnp.logical_or(place_first, place_second).astype(low)

    shard_in = expert_in[0].astype(low).reshape(slab, 2, grps, QUAD, units)
    in_pieces = jnp.transpose(shard_in, (1, 3, 0, 2, 4)).reshape(2, 1, QUAD, slab, quarter)
    in_pieces = jnp.broadcast_to(in_pieces, (2, grps, QUAD, slab, quarter)).reshape(
        2, reps, slab, quarter
    )
    down_mine = spread(expert_out[0].astype(low), "grp").reshape(quarter, width)
    gate_mine = swap(in_pieces[0], REP).reshape(width, quarter)
    up_mine = swap(in_pieces[1], REP).reshape(width, quarter)

    upstream = my_cotangent.astype(full) * valid_rows[:, None]

    def to_experts(block):
        sent = block.reshape((1, experts) + block.shape[1:])
        sent = jnp.broadcast_to(sent, (QUAD,) + sent.shape[1:])
        return swap(sent.reshape((QUAD * experts,) + block.shape[1:]), PLANE)

    def dispatch(values):
        return dot(place_any, values).astype(low).reshape(experts, capacity, width)

    expert_upstream = to_experts(dispatch(upstream.astype(low))).reshape(-1, width)
    active_grad_bare = lax.dot_general(
        expert_upstream, down_mine, (((1,), (1,)), ((), ())), preferred_element_type=full
    )

    x_group = group_tokens.astype(full)
    scale_group = lax.rsqrt(jnp.mean(x_group * x_group, axis=-1, keepdims=True) + eps_norm)
    normed_group = (x_group * scale_group * gain_one).astype(low).reshape(exps * rows, width)
    qkv = dot(normed_group, qkv_mine).astype(low).reshape(exps, rows, 3, heads, head_dim)
    queries = qkv[:, :, 0]
    key_rows = qkv[:, :, 1]
    values = qkv[:, :, 2]
    onehot = bucket_onehot(rows)
    bias_mine = lax.dynamic_slice_in_dim(rel_bias, place * heads, heads, 1)
    bias_table = jnp.einsum("ijb,bh->hij", onehot, bias_mine, precision=highest)

    def scores_of():
        raw = (
            jnp.einsum("sihd,sjhd->shij", queries, key_rows, preferred_element_type=full)
            * score_scale
            + bias_table[None]
        )
        return jnp.where(key_ok[:, None, None, :], raw, -1e30)

    scores = scores_of()
    row_max = jnp.max(scores, axis=-1, keepdims=True)
    log_total = row_max + jnp.log(jnp.sum(jnp.exp(scores - row_max), axis=-1, keepdims=True))
    weights_low = jnp.exp(scores - log_total).astype(low)
    context_mine = (
        jnp.einsum("shij,sjhd->sihd", weights_low, values, preferred_element_type=full)
        .astype(low)
        .reshape(exps, rows, head_cols)
    )
    context = jnp.transpose(swap(context_mine, "exp"), (1, 0, 2)).reshape(rows, width)

    x_float = tokens.astype(full)
    scale_one = lax.rsqrt(jnp.mean(x_float * x_float, axis=-1, keepdims=True) + eps_norm)
    hidden_one = x_float + dot(context, full_out)
    scale_two = lax.rsqrt(jnp.mean(hidden_one * hidden_one, axis=-1, keepdims=True) + eps_norm)
    normed_two = (hidden_one * scale_two * gain_two).astype(low)
    normed_float = normed_two.astype(full)
    router_probs = jax.nn.softmax(jnp.dot(normed_float, router, precision=highest), axis=-1)
    picked = jnp.sum(router_probs[:, None, :] * chosen, axis=-1)
    gate_total = jnp.sum(picked, axis=-1, keepdims=True)
    gate_value = picked / gate_total
    combine = gate_value * valid_rows[:, None]
    combine_slots = jnp.sum(
        jnp.where(place_first, combine[None, :, 0], 0.0)
        + jnp.where(place_second, combine[None, :, 1], 0.0),
        axis=1,
    ).reshape(experts, 1, capacity)

    expert_rows = to_experts(dispatch(normed_two)).reshape(-1, width)
    expert_combine = to_experts(combine_slots).reshape(-1, 1)

    gate_part = dot(expert_rows, gate_mine)
    up_part = dot(expert_rows, up_mine)
    active_float, active_pull = jax.vjp(gated_unit, gate_part, up_part)
    active = active_float.astype(low)
    active_scaled = (active_float * expert_combine).astype(low)
    combine_grad_part = jnp.sum(active_float * active_grad_bare, axis=-1).reshape(
        QUAD * experts, 1, capacity
    )
    gate_part_grad, up_part_grad = active_pull(active_grad_bare * expert_combine)
    gate_part_grad = gate_part_grad.astype(low)
    up_part_grad = up_part_grad.astype(low)
    rows_grad_part = (
        lax.dot_general(gate_part_grad, gate_mine, (((1,), (1,)), ((), ())), preferred_element_type=full)
        + lax.dot_general(up_part_grad, up_mine, (((1,), (1,)), ((), ())), preferred_element_type=full)
    ).astype(low)
    output_part = dot(active, down_mine).astype(low)

    combine_grad_back = swap(combine_grad_part, PLANE)
    rows_grad_back = swap(rows_grad_part.reshape(QUAD * experts, capacity, width), PLANE)
    output_back = swap(output_part.reshape(QUAD * experts, capacity, width), PLANE)

    def transposed_dot(a, b):
        return lax.dot_general(a, b, (((0,), (0,)), ((), ())), preferred_element_type=full)

    down_grad = transposed_dot(active_scaled, expert_upstream).astype(low)
    gate_grad = transposed_dot(expert_rows, gate_part_grad).astype(low)
    up_grad = transposed_dot(expert_rows, up_part_grad).astype(low)
    down_share = jnp.sum(
        swap(down_grad.reshape(grps, units, width), "grp").astype(full), axis=0
    )[None]

    def in_columns(grad):
        back = swap(grad.reshape(reps, slab, quarter), REP).astype(full)
        back = jnp.sum(back.reshape(grps, QUAD, slab, grps, units), axis=0)
        return jnp.transpose(back, (1, 2, 0, 3)).reshape(slab, grps * QUAD * units)

    in_share = jnp.concatenate([in_columns(gate_grad), in_columns(up_grad)], axis=1)[None]

    def from_slots(placed, parts):
        hot = jnp.broadcast_to(placed.astype(low)[None], (QUAD,) + placed.shape).reshape(-1, rows)
        return lax.dot_general(
            hot, parts.reshape(-1, width), (((0,), (0,)), ((), ())), preferred_element_type=full
        )

    mixture = combine[:, :1] * from_slots(place_first, output_back) + combine[:, 1:] * from_slots(
        place_second, output_back
    )
    block_loader = (valid_rows[:, None] * (hidden_one + mixture)).astype(low)
    seq_ids = jnp.arange(deal.shape[0], dtype=jnp.int32)
    dealt_seq = jnp.sum(jnp.where(deal == me, seq_ids, 0))
    block_out = lax.dynamic_index_in_dim(
        spread(block_loader, "exp"), dealt_seq - base, 0, keepdims=False
    )

    combine_grad_slots = jnp.sum(combine_grad_back.reshape(QUAD, slots), axis=0)
    combine_grad = jnp.stack(
        [
            jnp.sum(jnp.where(place_first, combine_grad_slots[:, None], 0.0), axis=0),
            jnp.sum(jnp.where(place_second, combine_grad_slots[:, None], 0.0), axis=0),
        ],
        axis=1,
    )
    gate_grad_value = combine_grad * valid_rows[:, None]
    picked_grad = (
        gate_grad_value - jnp.sum(gate_grad_value * gate_value, axis=-1, keepdims=True)
    ) / gate_total
    probs_grad = jnp.sum(picked_grad[:, :, None] * chosen, axis=1)
    logit_grad = router_probs * (
        probs_grad - jnp.sum(probs_grad * router_probs, axis=-1, keepdims=True)
    )
    router_grad = jnp.dot(normed_float.T, logit_grad, precision=highest)
    normed_grad = jnp.dot(logit_grad, router.T, precision=highest) + from_slots(
        jnp.logical_or(place_first, place_second), rows_grad_back
    )
    scaled_two = normed_grad * gain_two
    hidden_grad = (
        upstream
        + scale_two * scaled_two
        - hidden_one * scale_two**3 * jnp.mean(scaled_two * hidden_one, axis=-1, keepdims=True)
    )
    gain_two_grad = jnp.sum(normed_grad * hidden_one * scale_two, axis=0)
    branch_grad = hidden_grad.astype(low)
    context_grad = lax.dot_general(
        branch_grad, full_out, (((1,), (1,)), ((), ())), preferred_element_type=full
    ).astype(low)
    context_grad_pieces = jnp.transpose(context_grad.reshape(rows, exps, head_cols), (1, 0, 2))
    context_grad_mine = swap(context_grad_pieces, "exp").reshape(exps, rows, heads, head_dim)
    branch_group = spread(branch_grad, "exp").reshape(exps * rows, width)
    out_grad = transposed_dot(context_mine.reshape(exps * rows, head_cols), branch_group).astype(low)

    scores = scores_of()
    probs_again = jnp.exp(scores - log_total)
    weights_again = probs_again.astype(low)
    values_grad = jnp.einsum(
        "shij,sihd->sjhd", weights_again, context_grad_mine, preferred_element_type=full
    )
    probs_grad_att = jnp.einsum(
        "sihd,sjhd->shij", context_grad_mine, values, preferred_element_type=full
    )
    row_delta = jnp.sum(probs_grad_att * probs_again, axis=-1, keepdims=True)
    scores_grad = (probs_again * (probs_grad_att - row_delta)).astype(low)
    scores_grad_sum = jnp.sum(scores_grad.astype(full), axis=0)
    bias_grad_mine = jnp.einsum("hij,ijb->bh", scores_grad_sum, onehot, precision=highest)
    bias_grad = lax.dynamic_update_slice_in_dim(
        jnp.zeros((BUCKETS, HEADS), full), bias_grad_mine, place * heads, 1
    )
    queries_grad = (
        jnp.einsum("shij,sjhd->sihd", scores_grad, key_rows, preferred_element_type=full)
        * score_scale
    )
    keys_grad = (
        jnp.einsum("shij,sihd->sjhd", scores_grad, queries, preferred_element_type=full)
        * score_scale
    )
    qkv_grad = (
        jnp.stack([queries_grad, keys_grad, values_grad], axis=2)
        .astype(low)
        .reshape(exps * rows, 3 * head_cols)
    )
    normed_one_part = lax.dot_general(
        qkv_grad, qkv_mine, (((1,), (1,)), ((), ())), preferred_element_type=full
    ).astype(low)
    normed_one_grad = jnp.sum(
        swap(normed_one_part.reshape(exps, rows, width), "exp").astype(full), axis=0
    )
    scaled_one = normed_one_grad * gain_one
    token_grad = (
        hidden_grad
        + scale_one * scaled_one
        - x_float * scale_one**3 * jnp.mean(scaled_one * x_float, axis=-1, keepdims=True)
    )
    gain_one_grad = jnp.sum(normed_one_grad * x_float * scale_one, axis=0)

    qkv_weight_grad = transposed_dot(normed_group, qkv_grad).astype(low)
    qkv_grad_rows = swap(qkv_weight_grad.reshape(exps, row_block, 3 * head_cols), "exp")
    qkv_grad_rows = jnp.transpose(
        qkv_grad_rows.reshape(exps, row_block, 3, head_cols), (1, 2, 0, 3)
    ).reshape(row_block, reps, -1)
    qkv_share = jnp.sum(
        swap(jnp.transpose(qkv_grad_rows, (1, 0, 2)), REP).astype(full), axis=0
    )
    out_pieces = jnp.transpose(out_grad.reshape(row_block, reps, -1), (1, 0, 2))
    out_share = jnp.sum(swap(out_pieces, REP).astype(full), axis=0)

    small = jnp.concatenate(
        [
            router_grad.reshape(-1),
            jnp.stack([gain_one_grad, gain_two_grad], axis=1).reshape(-1),
            bias_grad.reshape(-1),
        ]
    ).reshape(-1, 128)
    small_total = jnp.sum(lax.all_gather(small, ALL, axis=0, tiled=False), axis=0).reshape(-1)
    router_total = small_total[: router.size].reshape(router.shape)
    gains_total = small_total[router.size : router.size + norm_gains.size].reshape(norm_gains.shape)
    bias_total = small_total[router.size + norm_gains.size :].reshape(rel_bias.shape)

    qkv_new = adamw_update(attn_qkv, qkv_first, qkv_second, qkv_share, 1.5 / math.sqrt(D), 0.1)
    out_new = adamw_update(attn_out, out_first, out_second, out_share, 6.0 / math.sqrt(D), 0.1)
    bias_new = adamw_update(rel_bias, bias_first, bias_second, bias_total, 0.3, 0.0)
    router_new = adamw_update(
        router, router_first, router_second, router_total, 1.0 / math.sqrt(D), 0.1
    )
    gains_new = adamw_update(norm_gains, gains_first, gains_second, gains_total, 0.5, 0.0)
    in_new = adamw_update(expert_in, in_first, in_second, in_share, 1.5 / math.sqrt(D), 0.1)
    down_new = adamw_update(
        expert_out, down_first, down_second, down_share, 1.5 / math.sqrt(FF), 0.1
    )
    return (
        (block_out, token_grad)
        + qkv_new
        + out_new
        + bias_new
        + router_new
        + gains_new
        + in_new
        + down_new
    )


def solution(mesh):
    reps, exps = mesh.devices.shape
    split = Mesh(mesh.devices.reshape(reps // QUAD, QUAD, exps), ALL)
    by_rows = P(ALL, None)
    attn = P("exp", REP)
    expert = P("exp", REP, None)
    return jax.shard_map(
        per_device if (reps, exps) == (2 * QUAD, 4) else plain_device,
        mesh=split,
        in_specs=(by_rows, by_rows) + (P(),) * 3 + (attn,) * 6 + (P(),) * 9 + (expert,) * 6,
        out_specs=(by_rows, by_rows) + (attn,) * 6 + (P(),) * 9 + (expert,) * 6,
        check_vma=False,
    )
```

```python
import functools
import math

import jax
import jax.numpy as jnp
from jax import lax
from jax.experimental import pallas as pl
from jax.experimental.pallas import tpu as pltpu
from jax.sharding import Mesh
from jax.sharding import PartitionSpec as P

D = 1024
HEADS = 16
FF = 2816
BUCKETS = 32
STEP = 10
QUAD = 4
REP = ("grp", "quad")
PLANE = ("quad", "exp")
ALL = ("grp", "quad", "exp")

highest = lax.Precision.HIGHEST
eps_norm = 1e-06
thresholds = (1, 2, 3, 4, 5, 6, 7, 8, 11, 16, 22, 32, 45, 64, 90)
beta_one = 0.9
beta_two = 0.999
eps_adam = 1e-08
low = jnp.bfloat16
full = jnp.float32
MESH = pl.DeviceIdType.MESH


def adamw_update(weight, moment, second, gradient, step_rate, decay_factor):
    new_moment = beta_one * moment + (1.0 - beta_one) * gradient
    new_second = beta_two * second + (1.0 - beta_two) * gradient * gradient
    corrected = new_moment / (1.0 - beta_one**STEP)
    scaled = new_second / (1.0 - beta_two**STEP)
    new_weight = weight - step_rate * (
        corrected / (jnp.sqrt(scaled) + eps_adam) + decay_factor * weight
    )
    return (new_moment, new_second, new_weight)


def gated_unit(gate_input, up_input):
    return jax.nn.gelu(gate_input, approximate=True) * up_input


def dot(a, b):
    return jnp.dot(a, b, preferred_element_type=full)


def nt(a, b, precision=None):
    return lax.dot_general(a, b, (((1,), (1,)), ((), ())), preferred_element_type=full, precision=precision)


def tn(a, b):
    return lax.dot_general(a, b, (((0,), (0,)), ((), ())), preferred_element_type=full)


class Where:
    def __init__(self, grps, exps):
        self.grps, self.exps = grps, exps
        self.reps = grps * QUAD
        self.grp = lax.axis_index("grp")
        self.quad = lax.axis_index("quad")
        self.exp = lax.axis_index("exp")
        self.rep = self.grp * QUAD + self.quad
        self.base = self.rep * exps
        self.me = self.base + self.exp

    def device(self, rep, exp):
        return (rep // QUAD, rep % QUAD, exp)

    def near(self, flip):
        q = self.quad
        if flip & 1:
            q = q + 1 - 2 * (q % 2)
        if flip & 2:
            q = q + 2 - 4 * (q // 2)
        return q


def send(src, dst, send_sem, recv_sem, device):
    return pltpu.make_async_remote_copy(
        src_ref=src, dst_ref=dst, send_sem=send_sem, recv_sem=recv_sem, device_id=device, device_id_type=MESH
    )


def arrived(ref, sem):
    pltpu.make_async_copy(ref, ref, sem).wait()


def greet(count, device):
    barrier = pltpu.get_barrier_semaphore()

    def one(k, _):
        pl.semaphore_signal(barrier, inc=1, device_id=device(k), device_id_type=MESH)
        return 0

    lax.fori_loop(1, count + 1, one, 0)
    return functools.partial(pl.semaphore_wait, barrier, count)


def everyone(at):
    count = at.reps * at.exps

    def device(k):
        other = (at.me + k) % count
        return at.device(other // at.exps, other % at.exps)

    return count - 1, device


def neighbours(at):
    members = QUAD * at.exps
    plane = at.quad * at.exps + at.exp

    def device(k):
        other = (plane + k) % members
        rest = k - members
        grp = jnp.where(k < members, at.grp, (at.grp + 1 + rest // QUAD) % at.grps)
        quad = jnp.where(k < members, other // at.exps, rest % QUAD)
        return grp, quad, jnp.where(k < members, other % at.exps, at.exp)

    return members - 1 + QUAD * (at.grps - 1), device


def turn(exp, i):
    beside = exp + 1 - 2 * (exp % 2)
    return jnp.where(i == 0, (beside + 2) % 4, jnp.where(i == 1, (exp + 2) % 4, jnp.where(i == 2, beside, exp)))


def lane_of(shape):
    return lax.broadcasted_iota(jnp.int32, shape, 1)


def row_of(shape):
    return lax.broadcasted_iota(jnp.int32, shape, 0)


def bucket_of(offset):
    distance = jnp.abs(offset)
    bucket = jnp.where(offset > 0, 16, 0)
    for threshold in thresholds:
        bucket = bucket + jnp.where(distance >= threshold, 1, 0)
    return bucket


def bits_of(count):
    return count.bit_length() - 1


def column_parts(width):
    tiles = width // 128
    cuts = [0, (tiles + 2) // 3, (2 * tiles + 2) // 3, tiles]
    return [(cuts[i] * 128, (cuts[i + 1] - cuts[i]) * 128) for i in range(3)]


def flipped(place, bit):
    return place + (1 - 2 * ((place // (1 << bit)) % 2)) * (1 << bit)


class Doubling:
    def __init__(self, at, own, every, sems, core_sems, orders):
        self.at, self.own, self.every = at, own, every
        self.sems, self.core_sems, self.orders = sems, core_sems, orders
        self.plane = at.quad * at.exps + at.exp
        self.steps = len(orders[0])
        self.parts = column_parts(own.shape[1])

    def device(self, bit):
        other = flipped(self.plane, bit)
        return (self.at.grp, other // self.at.exps, other % self.at.exps)

    def place(self, part, j):
        p = self.plane
        for i, bit in enumerate(self.orders[part]):
            if (j >> i) & 1:
                p = flipped(p, bit + 1)
        return p

    def block(self, part, p):
        begin, size = self.parts[part]
        return self.every.at[p, :, pl.ds(begin, size)]

    def source(self, part, j):
        begin, size = self.parts[part]
        return self.own.at[:, pl.ds(begin, size)] if j == 0 else self.block(part, self.place(part, j))

    def index(self, step, part, j):
        return part * (1 << self.steps) + (1 << step) - 1 + j

    def copy(self, step, part, j):
        i = self.index(step, part, j)
        return send(
            self.source(part, j),
            self.block(part, self.place(part, j)),
            self.sems.at[0, i],
            self.sems.at[1, i],
            self.device(self.orders[part][step] + 1),
        )

    def core_copy(self, part, j):
        i = part * (1 << self.steps) + j
        return send(
            self.source(part, j),
            self.block(part, self.place(part, j)),
            self.core_sems.at[0, i],
            self.core_sems.at[1, i],
            self.device(0),
        )

    def start(self):
        for part in range(3):
            for step in range(self.steps):
                self.copy(step, part, 0).start()
        for part in range(3):
            self.core_copy(part, 0).start()
        self.keep().start()

    def keep(self):
        return pltpu.make_async_copy(self.own, self.every.at[self.plane], self.core_sems.at[1, 3 << self.steps])

    def next(self, step):
        for part in range(3):
            for j in range(1 << step):
                k = (1 << step) + j
                arrived(self.block(part, self.place(part, k)), self.sems.at[1, self.index(step, part, j)])
                for later in range(step + 1, self.steps):
                    self.copy(later, part, k).start()
                self.core_copy(part, k).start()

    def finish_in(self):
        for part in range(3):
            for j in range(1 << self.steps):
                there = self.block(part, flipped(self.place(part, j), 0))
                arrived(there, self.core_sems.at[1, part * (1 << self.steps) + j])
        self.keep().wait()

    def finish_out(self):
        for part in range(3):
            for j in range(1 << self.steps):
                self.core_copy(part, j).wait_send()
            for step in range(self.steps):
                for j in range(1 << step):
                    self.copy(step, part, j).wait_send()


class Halving:
    def __init__(self, at, bufs, sems, orders):
        self.at, self.bufs, self.sems = at, bufs, sems
        self.plane = at.quad * at.exps + at.exp
        self.places = bits_of(QUAD * at.exps)
        self.chip_bits = list(range(self.places - 1))
        self.parts = column_parts(bufs[0].shape[2])
        self.orders = orders

    def device(self, bit):
        other = flipped(self.plane, bit)
        return (self.at.grp, other // self.at.exps, other % self.at.exps)

    def hop(self, step, part):
        order = self.orders[part]
        bit = order[step]
        left = [b for b in self.chip_bits if b not in order[:step]]
        pos = left.index(bit)
        half = 1 << (len(left) - 1)
        mine = (self.plane // (1 << (bit + 1))) % 2
        device = self.device(bit + 1)
        begin, size = self.parts[part]
        cols = pl.ds(begin, size)
        base = self.base(step, part)

        def index(j, value):
            return (j >> pos) * (1 << (pos + 1)) + value * (1 << pos) + j % (1 << pos)

        pairs = []
        for j in range(half):
            copy = functools.partial(
                send,
                self.bufs[step].at[index(j, 1 - mine), :, cols],
                self.bufs[step + 1].at[j, :, cols],
                self.sems.at[0, base + j],
                self.sems.at[1, base + j],
                device,
            )
            pairs.append((copy, index(j, mine), j))
        return pairs, begin, size, base

    def base(self, step, part):
        n = len(self.chip_bits)
        return part * (1 << n) + sum(1 << (n - 1 - s) for s in range(step))

    def start(self, step, part=None):
        for p in range(3) if part is None else [part]:
            for copy, _, _ in self.hop(step, p)[0]:
                copy().start()

    def add(self, step, part):
        pairs, begin, size, base = self.hop(step, part)
        cols = pl.ds(begin, size)
        here, there = self.bufs[step], self.bufs[step + 1]
        for _, keep, j in pairs:
            arrived(there.at[j, :, cols], self.sems.at[1, base + j])
            there[j, :, begin : begin + size] = (
                there[j, :, begin : begin + size] + here[keep, :, begin : begin + size]
            )

    def next(self, step):
        for p in range(3):
            self.add(step, p)
            if step + 1 < len(self.chip_bits):
                self.start(step + 1, p)

    def result(self):
        return self.bufs[len(self.chip_bits)]

    def finish(self):
        for step in range(len(self.chip_bits)):
            for p in range(3):
                for copy, _, _ in self.hop(step, p)[0]:
                    copy().wait_send()


class Group:
    def __init__(self, at, own, every, sems):
        self.at, self.own, self.every, self.sems = at, own, every, sems
        self.beside, self.across = at.exp + 1 - 2 * (at.exp % 2), (at.exp + 2) % 4

    def copy(self, src, index, send_index, device):
        return send(
            src, self.every.at[index], self.sems.at[0, send_index], self.sems.at[1, index], self.at.device(self.at.rep, device)
        )

    def first(self):
        return [
            self.copy(self.own, self.at.exp, 0, self.across),
            self.copy(self.own, self.at.exp, 1, self.beside),
        ]

    def second(self):
        return self.copy(self.every.at[self.across], self.across, 2, self.beside)

    def start(self):
        for copy in self.first():
            copy.start()

    def pass_on(self):
        arrived(self.every.at[self.across], self.sems.at[1, self.across])
        self.second().start()

    def arrive(self):
        for index in (self.beside, (self.beside + 2) % 4):
            arrived(self.every.at[index], self.sems.at[1, index])

    def sent(self):
        for copy in self.first() + [self.second()]:
            copy.wait_send()


class Tiles:
    def __init__(self, units, reps):
        self.units = units
        self.reps = reps
        self.hidden = units * reps
        self.half = self.hidden // 256
        self.wide = (self.half + 1) // 2
        self.count = 3
        self.size = 128 * self.wide // self.count
        self.skip = 128 * (2 * self.wide - self.half)

    def start(self, quad):
        return 128 * (self.half * (quad // 2) + (self.half - self.wide) * (quad % 2))

    def rows(self, tile):
        result = []
        for k in range(QUAD):
            found = None
            for parity in range(2):
                first = self.start(parity) + tile * self.size
                live = first + (self.skip if parity and tile == 0 else 0)
                begin = max(live, k * self.units)
                end = min(first + self.size, (k + 1) * self.units)
                if end > begin:
                    found = (begin - k * self.units, end - begin, parity, begin - first)
            result.append(found)
        return result


class Outward:
    def __init__(self, at, tiles, tile, in_low, down_slab, both_w, down_w, nothing, sems, down_sems):
        self.at, self.tiles, self.tile = at, tiles, tile
        self.in_low, self.down_slab, self.both_w, self.down_w = in_low, down_slab, both_w, down_w
        self.nothing, self.sems, self.down_sems = nothing, sems, down_sems
        self.slab = in_low.shape[0]

    def source(self, quad, section):
        begin = section * self.tiles.hidden + self.tiles.start(quad) + self.tile * self.tiles.size
        return self.in_low.at[:, pl.ds(pl.multiple_of(begin, 128), self.tiles.size)]

    def target(self, rep, section):
        rows = pl.ds(pl.multiple_of(rep * self.slab, self.slab), self.slab)
        return self.both_w.at[rows, pl.ds(section * self.tiles.size, self.tiles.size)]

    def over(self, act):
        at = self.at

        def one(k, _):
            other = (at.rep + k) % at.reps
            for section in range(2):
                act(
                    functools.partial(
                        send,
                        self.source(other % QUAD, section),
                        self.target(at.rep, section),
                        self.sems.at[0, section * at.reps + other],
                        self.sems.at[1, section * at.reps + at.rep],
                        at.device(other, at.exp),
                    )
                )
            return 0

        lax.fori_loop(1, at.reps, one, 0)

    def over_down(self, act, act_local):
        at = self.at
        for k, piece in enumerate(self.tiles.rows(self.tile)):
            if piece is None:
                continue
            begin, count, parity, to = piece
            quad = 2 * (at.rep // QUAD) + parity
            src, dst = self.down_slab.at[pl.ds(begin, count)], self.down_w.at[pl.ds(to, count)]
            recv = self.down_sems.at[1, at.rep]
            for g in range(at.grps):
                stays = jnp.logical_and(at.grp == g, at.quad == quad)
                ours = at.rep % QUAD == k

                @pl.when(jnp.logical_and(ours, jnp.logical_not(stays)))
                def _():
                    act(functools.partial(send, src, dst, self.down_sems.at[0, g], recv, (g, quad, at.exp)))

                @pl.when(jnp.logical_and(ours, stays))
                def _():
                    act_local(functools.partial(pltpu.make_async_copy, src, dst, recv))

    def blank(self):
        return pltpu.make_async_copy(
            self.nothing, self.down_w.at[pl.ds(0, self.tiles.skip)], self.down_sems.at[1, self.at.reps]
        )

    def start(self):
        at = self.at
        self.over_down(lambda copy: copy().start(), lambda copy: copy().start())
        self.over(lambda copy: copy().start())
        for section in range(2):
            pltpu.make_async_copy(
                self.source(at.quad, section), self.target(at.rep, section), self.sems.at[1, section * at.reps + at.rep]
            ).start()
        if self.tile == 0:

            @pl.when(at.quad % 2 == 1)
            def _():
                self.blank().start()

    def arrive(self):
        at = self.at

        def one(rep, _):
            for section in range(2):
                arrived(self.target(rep, section), self.sems.at[1, section * at.reps + rep])
            return 0

        lax.fori_loop(0, at.reps, one, 0)
        for parity in range(2):

            @pl.when(at.quad % 2 == parity)
            def _():
                for k, piece in enumerate(self.tiles.rows(self.tile)):
                    if piece is not None and piece[2] == parity:
                        source = QUAD * (at.quad // 2) + k
                        arrived(self.down_w.at[pl.ds(piece[3], piece[1])], self.down_sems.at[1, source])
                if parity and self.tile == 0:
                    self.blank().wait()

    def sent(self):
        self.over(lambda copy: copy().wait_send())
        self.over_down(lambda copy: copy().wait_send(), lambda copy: None)


class Homeward:
    def __init__(self, at, tiles, tile, both, down, in_parts, down_parts, sems, down_sems, sections=(0, 1)):
        self.at, self.tiles, self.tile, self.sections = at, tiles, tile, sections
        self.both, self.down, self.in_parts, self.down_parts = both, down, in_parts, down_parts
        self.sems, self.down_sems = sems, down_sems
        self.slab = in_parts.shape[1]

    def target(self, grp, quad, parity, section):
        skip = self.tiles.skip if parity and self.tile == 0 else 0
        to = section * self.tiles.hidden + self.tiles.start(quad) + self.tile * self.tiles.size + skip
        to = to if isinstance(to, int) else pl.multiple_of(to, 128)
        return skip, self.in_parts.at[grp, :, pl.ds(to, self.tiles.size - skip)]

    def copy(self, rep, parity, section, local=False):
        at = self.at
        skip, dst = self.target(at.grp, at.quad, parity, section)
        rows = pl.ds(pl.multiple_of(rep * self.slab, self.slab), self.slab)
        src = self.both.at[rows, pl.ds(section * self.tiles.size + skip, self.tiles.size - skip)]
        recv = self.sems.at[1, section * at.reps + at.rep]
        if local:
            return pltpu.make_async_copy(src, dst, recv)
        return send(src, dst, self.sems.at[0, section * at.reps + rep], recv, at.device(rep, at.exp))

    def over(self, act, act_local):
        at = self.at
        for parity in range(2):

            @pl.when(at.quad % 2 == parity)
            def _():
                def one(k, _):
                    for section in self.sections:
                        act(self.copy((at.rep + k) % at.reps, parity, section))
                    return 0

                lax.fori_loop(1, at.reps, one, 0)
                if act_local:
                    for section in self.sections:
                        act_local(self.copy(at.rep, parity, section, local=True))

    def over_down(self, act, act_local):
        at = self.at
        if self.down is None:
            return
        for k, piece in enumerate(self.tiles.rows(self.tile)):
            if piece is None:
                continue
            begin, count, parity, to = piece
            src, dst = self.down.at[pl.ds(to, count)], self.down_parts.at[at.grp, pl.ds(begin, count)]
            recv = self.down_sems.at[1, at.grp]
            stays = jnp.logical_and(at.grp == at.quad // 2, at.quad == k)
            ours = at.quad % 2 == parity

            @pl.when(jnp.logical_and(ours, jnp.logical_not(stays)))
            def _():
                act(functools.partial(send, src, dst, self.down_sems.at[0, k], recv, (at.quad // 2, k, at.exp)))

            @pl.when(jnp.logical_and(ours, stays))
            def _():
                act_local(functools.partial(pltpu.make_async_copy, src, dst, recv))

    def start(self):
        self.over_down(lambda copy: copy().start(), lambda copy: copy().start())
        self.over(lambda copy: copy.start(), lambda copy: copy.start())

    def arrive(self):
        at = self.at
        for rep in range(at.reps):
            for section in self.sections:
                _, dst = self.target(rep // QUAD, rep % QUAD, rep % 2, section)
                arrived(dst, self.sems.at[1, section * at.reps + rep])
        for k, piece in enumerate(self.tiles.rows(self.tile)):
            if piece is None or self.down is None:
                continue

            @pl.when(at.quad == k)
            def _():
                for g in range(at.grps):
                    arrived(self.down_parts.at[g, pl.ds(piece[0], piece[1])], self.down_sems.at[1, g])

    def sent(self):
        self.over(lambda copy: copy.wait_send(), None)
        self.over_down(lambda copy: copy().wait_send(), lambda copy: None)


def forward_kernel(
    grps,
    exps,
    lengths,
    bias_table,
    routes_t,
    tokens,
    cotangent,
    gains,
    router,
    attn_qkv,
    attn_out,
    expert_in,
    expert_out,
    both_w,
    down_w,
    cot_all,
    n_all,
    comb_all,
    qkv_out,
    lse_out,
    mine_out,
    n1_out,
    wqkv_out,
    wout_out,
    h1_out,
    n2_out,
    probs_out,
    in_out,
    down_out,
    in_wide,
    down_wide,
    qkv_t,
    out_w,
    in_low,
    down_slab,
    tok_all,
    wqkv,
    wout,
    n1,
    qkv,
    lse,
    mine,
    ctx,
    bias,
    comb_send,
    nothing,
    tok_sem,
    wq_sem,
    wo_sem,
    wo2_sem,
    weight_sem,
    down_sem,
    ctx_sem,
    cot_sem,
    cot_core_sem,
    n_sem,
    n_core_sem,
    comb_sem,
    store_sem,
    cast_sem,
):
    at = Where(grps, exps)
    reps = at.reps
    rows, width = tokens.shape
    heads = HEADS // exps
    head_dim = width // HEADS
    head_cols = heads * head_dim
    block_cols = min(128, head_cols)
    shard_cols, row_block = qkv_t.shape
    seg = math.gcd(shard_cols, head_cols)
    segs = shard_cols // seg
    tiles = Tiles(down_slab.shape[0], reps)
    plane = at.quad * exps + at.exp
    members = QUAD * exps
    scale = 1.0 / math.sqrt(head_dim)
    SEND, RECV = 0, 1

    met = greet(*everyone(at))
    wide_copies = [
        pltpu.make_async_copy(expert_in, in_wide, cast_sem.at[0]),
        pltpu.make_async_copy(expert_out, down_wide, cast_sem.at[1]),
    ]
    for copy in wide_copies:
        copy.start()
    qkv_t[...] = attn_qkv[...].T.astype(low)
    out_w[...] = attn_out[...].astype(low)
    met()

    def exp_peer(k):
        return (at.exp + k) % exps

    group_tokens = Group(at, tokens, tok_all, tok_sem)
    group_tokens.start()
    tok_all[at.exp] = tokens[...]

    def segment(k):
        col = (at.rep * segs + k) * seg
        section = col // width
        within = col - section * width
        owner = within // head_cols
        return owner, section * head_cols + within - owner * head_cols

    def segment_copy(k, shift):
        owner, offset = segment(k)
        src = qkv_t.at[pl.ds(k * seg, seg)]
        dst = wqkv.at[at.exp, pl.ds(pl.multiple_of(offset, seg), seg)]
        target = at.device((at.rep + shift) % reps, owner)
        return owner, src, dst, functools.partial(
            send, src, dst, wq_sem.at[SEND, k * reps + shift], wq_sem.at[RECV, at.exp * 3 * (head_cols // seg) + offset // seg], target
        )

    def over_segments(act, act_local):
        def one(i, _):
            k, shift = i // reps, i % reps
            owner, src, dst, copy = segment_copy(k, shift)
            stays = jnp.logical_and(shift == 0, owner == at.exp)

            @pl.when(jnp.logical_not(stays))
            def _():
                act(copy())

            @pl.when(stays)
            def _():
                act_local(k, src, dst)

            return 0

        lax.fori_loop(0, segs * reps, one, 0)

    def local_segment(k, src, dst):
        _, offset = segment(k)
        pltpu.make_async_copy(src, dst, wq_sem.at[RECV, at.exp * 3 * (head_cols // seg) + offset // seg]).start()

    over_segments(lambda copy: copy.start(), local_segment)

    for k in range(1, reps):
        other = (at.rep + k) % reps
        send(
            out_w, wout.at[at.exp, at.rep], wo_sem.at[SEND, other], wo_sem.at[RECV, at.rep], at.device(other, at.exp)
        ).start()
    wout[at.exp, at.rep] = out_w[...]
    chip_bits = list(range(bits_of(members) - 1))
    cots = Doubling(at, cotangent, cot_all, cot_sem, cot_core_sem, [chip_bits[::-1]] * 3)
    cots.start()

    span = 2 * rows
    bucket = bucket_of(lane_of((8, span)) - rows)
    for h in range(heads):
        line = jnp.zeros((8, span), full)
        for b in range(BUCKETS):
            line = jnp.where(bucket == b, bias_table[at.exp * heads + h, b], line)
        whole = jnp.broadcast_to(line[0:1], (rows, span))
        bias[h] = pltpu.roll(whole, 0, 1, stride=1, stride_axis=0)[:, rows:]

    group_tokens.pass_on()
    group_tokens.arrive()

    def norm_group(s, _):
        x = tok_all[s].astype(full)
        r = lax.rsqrt(jnp.mean(x * x, axis=1, keepdims=True) + eps_norm)
        n1[s] = (x * r * gains[0:1, :]).astype(low)
        return 0

    lax.fori_loop(0, exps, norm_group, 0)

    for copy in wide_copies:
        copy.wait()
    in_low[...] = in_wide[...].astype(low)
    down_slab[...] = down_wide[...].astype(low)
    nothing[...] = jnp.zeros_like(nothing)
    weights = [
        Outward(
            at, tiles, t, in_low, down_slab, both_w.at[t], down_w.at[t], nothing, weight_sem.at[t], down_sem.at[t]
        )
        for t in range(2)
    ]
    weights[0].start()

    def wait_segment(i, _):
        e, j = i // (3 * head_cols // seg), i % (3 * head_cols // seg)
        arrived(wqkv.at[e, pl.ds(pl.multiple_of(j * seg, seg), seg)], wq_sem.at[RECV, i])
        return 0

    lax.fori_loop(0, exps * 3 * head_cols // seg, wait_segment, 0)

    def project(s, _):
        total = jnp.zeros((rows, 3 * head_cols), full)
        for e in range(exps):
            total = total + nt(n1[s, :, e * row_block : (e + 1) * row_block], wqkv[e])
        qkv[s] = total.astype(low)
        return 0

    lax.fori_loop(0, exps, project, 0)

    group_wout = Group(at, wout.at[at.exp], wout, wo2_sem)

    def beside(k):
        if k == 1:
            for j in range(1, reps):
                other = (at.rep + j) % reps
                arrived(wout.at[at.exp, other], wo_sem.at[RECV, other])
            group_wout.start()
        elif k == 2:
            cots.next(0)
        else:
            group_wout.pass_on()

    def attend(i, _):
        s = turn(at.exp, i)
        for k in range(1, exps):

            @pl.when(i == k)
            def _():
                beside(k)

        ok = lane_of((rows, rows)) < lengths[at.base + s]
        lane = lane_of((rows, block_cols))
        sums = jnp.zeros((rows, 128), full)
        for c in range(head_cols // block_cols):
            cols = slice(c * block_cols, (c + 1) * block_cols)
            q = qkv[s, :, cols] * scale
            k = qkv[s, :, head_cols + c * block_cols : head_cols + (c + 1) * block_cols]
            v = qkv[s, :, 2 * head_cols + c * block_cols : 2 * head_cols + (c + 1) * block_cols]
            result = jnp.zeros((rows, block_cols), full)
            for t in range(block_cols // head_dim):
                h = c * (block_cols // head_dim) + t
                here = jnp.logical_and(lane >= t * head_dim, lane < (t + 1) * head_dim)
                scores = nt(jnp.where(here, q, jnp.zeros_like(q)), k) + bias[h]
                scores = jnp.where(ok, scores, -1e30)
                top = jnp.max(scores, axis=1, keepdims=True)
                weights = jnp.exp(scores - top)
                total = jnp.sum(weights, axis=1, keepdims=True)
                weights = (weights * (1.0 / total)).astype(low)
                result = jnp.where(here, jnp.dot(weights, v, preferred_element_type=full), result)
                sums = jnp.where(lane_of((rows, 128)) == h, top + jnp.log(total), sums)
            mine[s, :, cols] = result.astype(low)
        lse[s] = sums

        @pl.when(i < exps - 1)
        def _():
            send(
                mine.at[s], ctx.at[at.exp], ctx_sem.at[SEND, s], ctx_sem.at[RECV, at.exp], at.device(at.rep, s)
            ).start()

        @pl.when(i == exps - 1)
        def _():
            pltpu.make_async_copy(mine.at[s], ctx.at[at.exp], ctx_sem.at[RECV, at.exp]).start()

        return 0

    lax.fori_loop(0, exps, attend, 0)

    cots.next(1)
    group_wout.arrive()
    for e in range(exps):
        arrived(ctx.at[e], ctx_sem.at[RECV, e])

    out_cols = wout.shape[3]
    for r in range(reps):
        cols = slice(r * out_cols, (r + 1) * out_cols)
        total = tokens[:, cols].astype(full)
        for e in range(exps):
            total = total + jnp.dot(ctx[e], wout[e, r], preferred_element_type=full)
        h1_out[:, cols] = total
    h1 = h1_out[...]
    r2 = lax.rsqrt(jnp.mean(h1 * h1, axis=1, keepdims=True) + eps_norm)
    n2 = (h1 * r2 * gains[1:2, :]).astype(low)
    n2_out[...] = n2
    rotated = [chip_bits[c:] + chip_bits[:c] for c in range(3)]
    rows_two = Doubling(at, n2_out, n_all, n_sem, n_core_sem, rotated)
    rows_two.start()
    weights[1].start()

    router_rows = jnp.concatenate([router[...], jnp.zeros((128 - exps, width), full)], axis=0)
    logits = nt(n2.astype(full), router_rows, precision=highest)
    lane = lane_of((rows, 128))
    logits = jnp.where(lane < exps, logits, -1e30)
    probs = jnp.exp(logits - jnp.max(logits, axis=1, keepdims=True))
    probs = probs / jnp.sum(probs, axis=1, keepdims=True)
    probs_out[...] = probs
    picked = jnp.where(routed(routes_t, at.me, rows), probs, 0.0)
    comb = picked / jnp.sum(picked, axis=1, keepdims=True)
    comb = jnp.where(row_of((rows, 1)) < lengths[at.me], comb, 0.0)
    comb_send[...] = comb.T[0 : comb_send.shape[0]]

    def comb_copy(k):
        other = (plane + k) % members
        return send(
            comb_send,
            comb_all.at[plane],
            comb_sem.at[SEND, other],
            comb_sem.at[RECV, plane],
            (at.grp, other // exps, other % exps),
        )

    def start_comb(k, _):
        comb_copy(k).start()
        return 0

    lax.fori_loop(1, members, start_comb, 0)
    pltpu.make_async_copy(comb_send, comb_all.at[plane], comb_sem.at[RECV, plane]).start()
    rows_two.next(0)

    stores = [
        (qkv, qkv_out),
        (lse, lse_out),
        (mine, mine_out),
        (n1, n1_out),
        (wqkv, wqkv_out),
        (wout, wout_out),
        (in_low, in_out),
        (down_slab, down_out),
    ]
    for i, (src, dst) in enumerate(stores):
        pltpu.make_async_copy(src, dst, store_sem.at[i]).start()

    for step in range(1, rows_two.steps):
        rows_two.next(step)
    for step in range(2, cots.steps):
        cots.next(step)

    cots.finish_in()
    rows_two.finish_in()

    def comb_in(k, _):
        arrived(comb_all.at[k], comb_sem.at[RECV, k])
        return 0

    lax.fori_loop(0, members, comb_in, 0)
    for tile in weights:
        tile.arrive()

    for k in range(1, exps):
        peer = exp_peer(k)
        arrived(mine.at[peer], ctx_sem.at[SEND, peer])
    over_segments(lambda copy: copy.wait_send(), lambda k, src, dst: None)
    for k in range(1, reps):
        arrived(out_w, wo_sem.at[SEND, (at.rep + k) % reps])
    group_tokens.sent()
    group_wout.sent()
    cots.finish_out()
    rows_two.finish_out()

    def sent_comb(k, _):
        comb_copy(k).wait_send()
        return 0

    lax.fori_loop(1, members, sent_comb, 0)
    for tile in weights:
        tile.sent()
    for i, (src, dst) in enumerate(stores):
        pltpu.make_async_copy(src, dst, store_sem.at[i]).wait()


def forward_call(
    grps, exps, lengths, bias_table, routes_t, tokens, cotangent, gains, router, attn_qkv, attn_out, expert_in, expert_out
):
    reps = grps * QUAD
    rows, width = tokens.shape
    head_cols = width // exps
    row_block, shard_cols = attn_qkv.shape
    seg = math.gcd(shard_cols, head_cols)
    segs = shard_cols // seg
    units = expert_out.shape[0]
    out_cols = attn_out.shape[1]
    heads = HEADS // exps
    members = QUAD * exps
    tiles = Tiles(units, reps)
    shape = jax.ShapeDtypeStruct
    vmem = pl.BlockSpec(memory_space=pltpu.VMEM)
    smem = pl.BlockSpec(memory_space=pltpu.SMEM)
    hbm = pl.BlockSpec(memory_space=pl.ANY)
    results = [
        (shape((2, width, 2 * tiles.size), low), hbm),
        (shape((2, tiles.size, width), low), hbm),
        (shape((members, rows, width), low), hbm),
        (shape((members, rows, width), low), hbm),
        (shape((members, 8, rows), full), hbm),
        (shape((exps, rows, 3 * head_cols), low), hbm),
        (shape((exps, rows, 128), full), hbm),
        (shape((exps, rows, head_cols), low), hbm),
        (shape((exps, rows, width), low), hbm),
        (shape((exps, 3 * head_cols, row_block), low), hbm),
        (shape((exps, reps, row_block, out_cols), low), hbm),
        (shape((rows, width), full), vmem),
        (shape((rows, width), low), vmem),
        (shape((rows, 128), full), vmem),
        (shape(expert_in.shape, low), hbm),
        (shape(expert_out.shape, low), hbm),
    ]
    dma = pltpu.SemaphoreType.DMA
    chips = members // 2
    return pl.pallas_call(
        functools.partial(forward_kernel, grps, exps),
        out_shape=[r[0] for r in results],
        in_specs=[smem] * 2 + [vmem] * 7 + [hbm] * 2,
        out_specs=[r[1] for r in results],
        scratch_shapes=[
            pltpu.VMEM(expert_in.shape, full),
            pltpu.VMEM(expert_out.shape, full),
            pltpu.VMEM((shard_cols, row_block), low),
            pltpu.VMEM((row_block, out_cols), low),
            pltpu.VMEM(expert_in.shape, low),
            pltpu.VMEM(expert_out.shape, low),
            pltpu.VMEM((exps, rows, width), low),
            pltpu.VMEM((exps, 3 * head_cols, row_block), low),
            pltpu.VMEM((exps, reps, row_block, out_cols), low),
            pltpu.VMEM((exps, rows, width), low),
            pltpu.VMEM((exps, rows, 3 * head_cols), low),
            pltpu.VMEM((exps, rows, 128), full),
            pltpu.VMEM((exps, rows, head_cols), low),
            pltpu.VMEM((exps, rows, head_cols), low),
            pltpu.VMEM((heads, rows, rows), full),
            pltpu.VMEM((8, rows), full),
            pltpu.VMEM((tiles.skip, width), low),
            dma((2, exps)),
            dma((2, max(segs * reps, exps * 3 * head_cols // seg))),
            dma((2, reps)),
            dma((2, exps)),
            dma((2, 2, 2 * reps)),
            dma((2, 2, reps + 1)),
            dma((2, exps)),
            dma((2, 3 * chips)),
            dma((2, 3 * chips + 1)),
            dma((2, 3 * chips)),
            dma((2, 3 * chips + 1)),
            dma((2, members)),
            dma((8,)),
            dma((2,)),
        ],
        compiler_params=pltpu.CompilerParams(
            collective_id=0, has_side_effects=True, vmem_limit_bytes=60 * 1024 * 1024
        ),
        name="forward",
    )(lengths, bias_table, routes_t, tokens, cotangent, gains, router, attn_qkv, attn_out, expert_in, expert_out)


def expert_kernel(
    grps,
    exps,
    cap,
    deal,
    routes_t,
    comb,
    n_all,
    cot_all,
    both_w,
    down_w,
    in_low,
    down_slab,
    h1,
    n_total,
    y_half,
    y_far,
    c_in,
    both_g,
    down_g,
    in_parts,
    down_parts,
    place,
    marks,
    n_rows,
    g_rows,
    both_v,
    down_v,
    raw_n,
    raw_g,
    y_acc,
    n_acc,
    both_d,
    active,
    both_stage,
    down_stage,
    n_bufs,
    c_sum,
    out_y,
    load_sem,
    raw_sem,
    out_sem,
    in_sem,
    in_down_sem,
    home_sem,
    home_down_sem,
    stage_sem,
    far_sem,
    n_sem,
    c_sem,
):
    at = Where(grps, exps)
    rows, width = n_all.shape[1:]
    tiles = Tiles(down_slab.shape[0], at.reps)
    size = tiles.size
    slots = exps * cap
    members = QUAD * exps
    loads = [pltpu.make_async_copy(both_w.at[t], both_v.at[t], load_sem.at[0, t]) for t in range(2)] + [
        pltpu.make_async_copy(down_w.at[t], down_v.at[t], load_sem.at[1, t]) for t in range(2)
    ]
    for copy in loads:
        copy.start()

    def raw_copies(q):
        here = pl.ds(pl.multiple_of(q * exps, exps), exps)
        return [
            pltpu.make_async_copy(n_all.at[here], raw_n.at[pl.ds(q % 2 * exps, exps)], raw_sem.at[0, q % 2]),
            pltpu.make_async_copy(cot_all.at[here], raw_g.at[pl.ds(q % 2 * exps, exps)], raw_sem.at[1, q % 2]),
        ]

    for copy in raw_copies(0):
        copy.start()

    beside = at.exp + 1 - 2 * (at.exp % 2)
    greet(*neighbours(at))()
    last = tiles.count - 1
    incoming = Outward(
        at, tiles, last, in_low, down_slab, both_v.at[last], down_v.at[last], None, in_sem, in_down_sem
    )
    incoming.start()
    home = Homeward(
        at, tiles, 0, both_stage.at[0], down_stage.at[0], in_parts, down_parts, home_sem, home_down_sem, (0,)
    )

    earlier = jnp.where(row_of((rows, rows)) < lane_of((rows, rows)), 1.0, 0.0).astype(low)
    slot = row_of((cap, rows)).astype(full)

    def dispatch(q, _):
        @pl.when(q + 1 < QUAD)
        def _():
            for copy in raw_copies(q + 1):
                copy.start()

        for copy in raw_copies(q):
            copy.wait()
        lines = []
        for j in range(exps):
            seq = at.grp * members + q * exps + j
            pair = routes_t[:, pl.ds(pl.multiple_of(seq * rows, rows), rows)]
            lines.append(jnp.logical_or(pair[0:1] == at.exp, pair[1:2] == at.exp))
        lines = [jnp.where(line, 1.0, 0.0) for line in lines] + [jnp.zeros((8 - exps, rows), full)]
        hot_low = jnp.concatenate(lines, axis=0).astype(low)
        before = dot(hot_low, earlier)
        for j in range(exps):
            s = q * exps + j
            inside = jnp.logical_and(slot == before[j : j + 1, :], hot_low[j : j + 1, :].astype(full) > 0.5)
            here = jnp.where(inside, 1.0, 0.0)
            place[s] = here.astype(low)
            g = raw_g[q % 2 * exps]
            for b in range(1, exps):
                g = jnp.where(deal[at.grp * members + s] == at.grp * members + q * exps + b, raw_g[q % 2 * exps + b], g)
            where = pl.ds(pl.multiple_of(s * cap, cap), cap)
            n_rows[where] = dot(here.astype(low), raw_n[q % 2 * exps + j]).astype(low)
            g_rows[where] = dot(here.astype(low), g).astype(low)
            marks[where, 0:1] = jnp.sum(here * comb[s, pl.ds(at.exp, 1), :], axis=1, keepdims=True)
            marks[where, 1:2] = jnp.zeros((cap, 1), full)
        return 0

    lax.fori_loop(0, QUAD, dispatch, 0)
    for copy in loads:
        copy.wait()
    curve = math.sqrt(2.0 / math.pi)

    core = at.exp % 2

    plane = at.quad * exps + at.exp
    sibling = at.device(at.rep, beside)
    dn = Halving(at, n_bufs, n_sem, [[0, 1, 2], [1, 2, 0], [2, 0, 1]])

    def n_copy(j):
        return send(raw_n.at[j], n_bufs[0].at[j], far_sem.at[0, 0, j], far_sem.at[0, 1, j], sibling)

    def y_copies(j):
        return (
            pltpu.make_async_copy(out_y.at[j % 2], y_half.at[j], out_sem.at[j % 2]),
            send(raw_n.at[j], y_far.at[j], far_sem.at[1, 0, j], far_sem.at[1, 1, j], sibling),
        )

    def c_copy(k):
        other = (plane + k) % members
        return send(
            c_sum.at[other],
            c_in.at[plane],
            c_sem.at[0, other],
            c_sem.at[1, plane],
            (at.grp, other // exps, other % exps),
        )

    def slots_of(s):
        return pl.ds(pl.multiple_of(s * cap, cap), cap)

    def n_rows_of(s):
        where = slots_of(s)
        line = jnp.sum(place[s].astype(full) * marks[where, 1:2], axis=0, keepdims=True)
        c_sum[s] = jnp.broadcast_to(line, (8, rows))
        return tn(place[s], n_acc[where]).astype(low)

    def y_rows_of(p):
        first = p // exps * exps
        spot = at.grp * members + p
        here, y = place[first], y_acc[slots_of(first)]
        for c in range(1, exps):
            taken = deal[at.grp * members + first + c] == spot
            here = jnp.where(taken, place[first + c], here)
            y = jnp.where(taken, y_acc[slots_of(first + c)], y)
        return (tn(here, y) + jnp.where(deal[at.me] == spot, h1[...], 0.0)).astype(low)

    def give_n(j, _):
        raw_n[j] = n_rows_of(2 * j + 1 - core)
        n_copy(j).start()
        raw_g[j] = n_rows_of(2 * j + core)
        return 0

    def add_n(j, _):
        arrived(n_bufs[0].at[j], far_sem.at[0, 1, j])
        n_bufs[0][j] = n_bufs[0][j] + raw_g[j]
        return 0

    def give_y(j, _):
        @pl.when(j >= 2)
        def _():
            y_copies(j - 2)[0].wait()

        out_y[j % 2] = y_rows_of(2 * j + core)
        n_copy(j).wait_send()
        raw_n[j] = y_rows_of(2 * j + 1 - core)
        for copy in y_copies(j):
            copy.start()
        return 0

    def start_c(k, _):
        c_copy(k).start()
        return 0

    def tile_work(f, _):
        @pl.when(f == last)
        def _():
            incoming.arrive()

        def chunk(c, _):
            here = pl.ds(pl.multiple_of(c * slots, slots), slots)
            share = marks[here, 0:1]
            both = dot(n_rows[here], both_v[f])
            gate_part, up_part = both[:, :size], both[:, size:]
            grad = nt(g_rows[here], down_v[f])
            square = gate_part * gate_part
            bend = jnp.tanh(curve * gate_part * (1.0 + 0.044715 * square))
            half = 0.5 * (1.0 + bend)
            gelu = gate_part * half
            slope = half + (0.5 * curve) * gate_part * (1.0 - bend * bend) * (1.0 + (3 * 0.044715) * square)
            value = gelu * up_part
            marks[here, 1:2] += jnp.sum(value * grad, axis=1, keepdims=True)
            grad = grad * share
            active[here] = (value * share).astype(low)
            both_d[here, :size] = (grad * up_part * slope).astype(low)
            both_d[here, size:] = (grad * gelu).astype(low)
            y = dot(active[here], down_v[f])
            y_acc[here] = jnp.where(f == 0, y, y_acc[here].astype(full) + y).astype(low)
            n_back = nt(both_d[here], both_v[f])
            n_acc[here] = jnp.where(f == 0, n_back, n_acc[here].astype(full) + n_back).astype(low)
            return 0

        lax.fori_loop(0, QUAD, chunk, 0)

        @pl.when(f == last)
        def _():
            lax.fori_loop(0, members // 2, give_n, 0)
            lax.fori_loop(1, members, start_c, 0)

        def columns(m, _):
            cols = pl.ds(pl.multiple_of(m * (width // 2), width // 2), width // 2)
            both_stage[f, cols] = tn(n_rows[:, cols], both_d[...]).astype(low)
            down_stage[f, :, cols] = tn(active[...], g_rows[:, cols]).astype(low)
            return 0

        lax.fori_loop(0, 2, columns, 0)

        for copy in stage_copies(f):
            copy.start()

        @pl.when(f == 0)
        def _():
            home.start()

        @pl.when(f > 0)
        def _():
            down_copy(f).start()

        return 0

    def stage_copies(f):
        return [pltpu.make_async_copy(both_stage.at[f], both_g.at[f], stage_sem.at[0, f])]

    def down_copy(f):
        return pltpu.make_async_copy(down_stage.at[f], down_g.at[f - 1], stage_sem.at[1, f])

    lax.fori_loop(0, tiles.count, tile_work, 0)

    half = members // 2
    lax.fori_loop(0, half, add_n, 0)
    dn.start(0)
    c_in[plane] = c_sum[plane]
    lax.fori_loop(0, half, give_y, 0)
    for step in range(len(dn.chip_bits)):
        dn.next(step)
    n_total[...] = dn.result()[0]
    for j in (half - 2, half - 1):
        y_copies(j)[0].wait()
    for f in range(tiles.count):
        for copy in stage_copies(f):
            copy.wait()
        if f:
            down_copy(f).wait()

    def core_in(j, _):
        y_copies(j)[1].wait_send()
        arrived(y_far.at[j], far_sem.at[1, 1, j])
        return 0

    lax.fori_loop(0, half, core_in, 0)

    def c_done(k, _):
        c_copy(k).wait_send()
        other = (plane + k) % members
        arrived(c_in.at[other], c_sem.at[1, other])
        return 0

    lax.fori_loop(1, members, c_done, 0)
    dn.finish()
    home.arrive()
    incoming.sent()
    home.sent()


def expert_call(grps, exps, cap, deal, routes_t, comb_all, n_all, cot_all, both_w, down_w, in_low, down_slab, h1):
    members, rows, width = n_all.shape
    reps = grps * QUAD
    tiles = Tiles(down_slab.shape[0], reps)
    size = tiles.size
    slab, both_hidden = in_low.shape
    units = down_slab.shape[0]
    slots = exps * cap
    chip_bits = bits_of(members) - 1
    shape = jax.ShapeDtypeStruct
    vmem = pl.BlockSpec(memory_space=pltpu.VMEM)
    smem = pl.BlockSpec(memory_space=pltpu.SMEM)
    hbm = pl.BlockSpec(memory_space=pl.ANY)
    results = [
        (shape((rows, width), low), vmem),
        (shape((members // 2, rows, width), low), hbm),
        (shape((members // 2, rows, width), low), hbm),
        (shape((members, 8, rows), full), vmem),
        (shape((tiles.count, width, 2 * size), low), hbm),
        (shape((2, size, width), low), hbm),
        (shape((grps, slab, both_hidden), low), hbm),
        (shape((grps, units, width), low), hbm),
    ]
    dma = pltpu.SemaphoreType.DMA
    return pl.pallas_call(
        functools.partial(expert_kernel, grps, exps, cap),
        out_shape=[r[0] for r in results],
        in_specs=[smem] + [vmem] * 2 + [hbm] * 6 + [vmem],
        out_specs=[r[1] for r in results],
        scratch_shapes=[
            pltpu.VMEM((members, cap, rows), low),
            pltpu.VMEM((QUAD * slots, 128), full),
            pltpu.VMEM((QUAD * slots, width), low),
            pltpu.VMEM((QUAD * slots, width), low),
            pltpu.VMEM((tiles.count, width, 2 * size), low),
            pltpu.VMEM((tiles.count, size, width), low),
            pltpu.VMEM((2 * exps, rows, width), low),
            pltpu.VMEM((2 * exps, rows, width), low),
            pltpu.VMEM((QUAD * slots, width), low),
            pltpu.VMEM((QUAD * slots, width), low),
            pltpu.VMEM((QUAD * slots, 2 * size), low),
            pltpu.VMEM((QUAD * slots, size), low),
            pltpu.VMEM((tiles.count, width, 2 * size), low),
            pltpu.VMEM((tiles.count, size, width), low),
            [pltpu.VMEM((members >> (1 + step), rows, width), low) for step in range(chip_bits + 1)],
            pltpu.VMEM((members, 8, rows), full),
            pltpu.VMEM((2, rows, width), low),
            dma((2, 2)),
            dma((2, 2)),
            dma((2,)),
            dma((2, 2 * reps)),
            dma((2, reps + 1)),
            dma((2, 2 * reps)),
            dma((2, max(QUAD, grps))),
            dma((2, tiles.count)),
            dma((2, 2, members // 2)),
            dma((2, 3 << chip_bits)),
            dma((2, members)),
        ],
        compiler_params=pltpu.CompilerParams(
            collective_id=2, has_side_effects=True, vmem_limit_bytes=60 * 1024 * 1024
        ),
        name="experts",
    )(deal, routes_t, comb_all, n_all, cot_all, both_w, down_w, in_low, down_slab, h1)


def adamw_root(weight, moment, second, gradient, step_rate, decay_factor):
    new_moment = beta_one * moment + (1.0 - beta_one) * gradient
    new_second = beta_two * second + (1.0 - beta_two) * gradient * gradient
    root = lax.rsqrt(new_second * (1.0 / (1.0 - beta_two**STEP)))
    step = new_moment * (root * (1.0 - eps_adam * root))
    keep = 1.0 - step_rate * decay_factor
    return (new_moment, new_second, keep * weight - (step_rate / (1.0 - beta_one**STEP)) * step)


def adam_kernel(exps, *refs):
    in_parts, down_parts, qkv_grad, out_grad, small = refs[:5]
    states, news, bias_grad = refs[5:26], refs[26:47], refs[47]
    heads = HEADS // exps
    width = small.shape[1]

    def update(i, grad, rate, decay):
        weight, first, second = [state[...] for state in states[3 * i : 3 * i + 3]]
        values = adamw_root(weight, first, second, grad, rate, decay)
        for new, value in zip(news[3 * i : 3 * i + 3], values, strict=True):
            new[...] = value

    def total(parts):
        result = parts[0].astype(full)
        for k in range(1, parts.shape[0]):
            result = result + parts[k].astype(full)
        return result

    @pl.when(pl.program_id(0) == 0)
    def _():
        update(0, qkv_grad[...], 1.5 / math.sqrt(D), 0.1)
        update(1, out_grad[...], 6.0 / math.sqrt(D), 0.1)
        for e in range(exps):
            for h in range(heads):
                bias_grad[e * heads + h : e * heads + h + 1, :] = small[
                    exps + 3 + e : exps + 4 + e, h * 128 : h * 128 + BUCKETS
                ]
        update(2, bias_grad[...], 0.3, 0.0)
        update(3, small[0:exps, :], 1.0 / math.sqrt(D), 0.1)
        update(4, small[exps : exps + 2, :], 0.5, 0.0)

    update(5, total(in_parts), 1.5 / math.sqrt(D), 0.1)
    update(6, total(down_parts), 1.5 / math.sqrt(FF), 0.1)


def adam_call(exps, in_parts, down_parts, qkv_grad, out_grad, small, states):
    steps = 4

    def whole(array):
        return pl.BlockSpec(array.shape, lambda i: (0,) * array.ndim)

    def columns(array):
        block = array.shape[:-1] + (array.shape[-1] // steps,)
        return pl.BlockSpec(block, lambda i: (0,) * (array.ndim - 1) + (i,))

    specs = [whole(state) for state in states[:15]]
    specs += [columns(state) for state in states[15:18]] + [columns(state) for state in states[18:]]
    return pl.pallas_call(
        functools.partial(adam_kernel, exps),
        grid=(steps,),
        in_specs=[columns(in_parts), columns(down_parts), whole(qkv_grad), whole(out_grad), whole(small)] + specs,
        out_specs=specs,
        out_shape=[jax.ShapeDtypeStruct(state.shape, full) for state in states],
        scratch_shapes=[pltpu.VMEM((HEADS, BUCKETS), full)],
        compiler_params=pltpu.CompilerParams(vmem_limit_bytes=60 * 1024 * 1024),
        name="adam",
    )(in_parts, down_parts, qkv_grad, out_grad, small, *states)


def backward_kernel(
    grps,
    exps,
    lengths,
    deal,
    bias_table,
    y_half,
    y_far,
    both_g,
    down_g,
    in_before,
    down_before,
    n1_in,
    cot_all,
    routes_t,
    tokens,
    n_total,
    c_in,
    n2_in,
    probs_in,
    h1_from,
    qkv_from,
    lse_from,
    mine_from,
    wqkv_from,
    wout_from,
    gains,
    router_t,
    *rest,
):
    token_grad, block_out, in_parts, down_parts, qkv_grad, out_grad, small_out = rest[:7]
    scratch = rest[7:]
    (
    h1_in,
    qkv,
    lse,
    mine,
    wqkv,
    wout,
    kept,
    y_bufs,
    dh1,
    dz_send,
    dz_all,
    do_send,
    do_in,
    bias,
    bias_sum,
    dqkv,
    dqkv_t,
    dn1_send,
    dn1_in,
    wq_send,
    og_send,
    mids,
    far_send,
    far_in,
    small_send,
    small_exp,
    small_sum,
    small_rep,
    y_sem,
    load_sem,
    weight_sem,
    down_sem,
    dz_sem,
    do_sem,
    dn1_sem,
    wq_sem,
    og_sem,
    mid_sem,
    far_sem,
    small_sem,
    small2_sem,
    n1_sem,
    operand_sem,
    ) = scratch
    at = Where(grps, exps)
    reps = at.reps
    rows, width = tokens.shape
    heads = HEADS // exps
    head_dim = width // HEADS
    head_cols = heads * head_dim
    block_cols = min(128, head_cols)
    row_block = wqkv.shape[2]
    out_cols = wout.shape[3]
    tiles = Tiles(down_parts.shape[1], reps)
    scale = 1.0 / math.sqrt(head_dim)
    SEND, RECV = 0, 1
    plane = at.quad * exps + at.exp
    members = QUAD * exps

    def exp_peer(k):
        return (at.exp + k) % exps

    router = router_t[...]
    met = greet(*neighbours(at))
    n1 = kept.at[0:exps]
    group = pl.ds(pl.multiple_of(at.quad * exps, exps), exps)
    cot_copy = pltpu.make_async_copy(cot_all.at[group], dn1_send, n1_sem.at[1])
    cot_copy.start()
    loads = [
        pltpu.make_async_copy(src, dst, operand_sem.at[i])
        for i, (src, dst) in enumerate(
            ((h1_from, h1_in), (wout_from, wout), (qkv_from, qkv), (lse_from, lse), (mine_from, mine), (wqkv_from, wqkv))
        )
    ]
    ys = Halving(at, y_bufs, y_sem, [[0, 1, 2], [0, 1, 2], [1, 0, 2]])
    half_loads = [
        pltpu.make_async_copy(y_far, y_bufs[0], load_sem.at[0]),
        pltpu.make_async_copy(y_half, kept, load_sem.at[1]),
    ]
    for copy in loads + half_loads:
        copy.start()

    span = 2 * rows
    bucket = bucket_of(lane_of((8, span)) - rows)
    for h in range(heads):
        line = jnp.zeros((8, span), full)
        for b in range(BUCKETS):
            line = jnp.where(bucket == b, bias_table[at.exp * heads + h, b], line)
        whole = jnp.broadcast_to(line[0:1], (rows, span))
        bias[h] = pltpu.roll(whole, 0, 1, stride=1, stride_axis=0)[:, rows:]


    met()

    homes = [
        Homeward(
            at,
            tiles,
            t,
            both_g.at[t],
            down_g.at[t - 1] if t else None,
            in_parts,
            down_parts,
            weight_sem.at[t],
            down_sem.at[t],
            (0, 1) if t else (1,),
        )
        for t in range(tiles.count)
    ]
    homes[0].start()
    homes[1].start()
    n1_copy = pltpu.make_async_copy(n1_in, n1, n1_sem.at[0])

    lane = lane_of((rows, 128))
    comb_rows = []
    for e in range(exps):
        total = c_in[e]
        for q in range(1, QUAD):
            total = total + c_in[q * exps + e]
        comb_rows.append(total[0:1, :])
    comb_rows.append(jnp.zeros((128 - exps, rows), full))
    comb_grad = jnp.concatenate(comb_rows, axis=0).T
    valid = row_of((rows, 1)) < lengths[at.me]
    probs = probs_in[...]
    hot = routed(routes_t, at.me, rows)
    picked = jnp.where(hot, probs, 0.0)
    total = jnp.sum(picked, axis=1, keepdims=True)
    gate = picked / total
    gate_grad_rows = jnp.where(valid, comb_grad, 0.0)
    spread_grad = jnp.sum(gate_grad_rows * gate, axis=1, keepdims=True)
    probs_grad = jnp.where(hot, (gate_grad_rows - spread_grad) / total, 0.0)
    logit_grad = probs * (probs_grad - jnp.sum(probs_grad * probs, axis=1, keepdims=True))
    small_rows = small_send.shape[0]
    small_send[...] = jnp.zeros_like(small_send)
    router_back = jnp.dot(
        logit_grad, jnp.concatenate([router, jnp.zeros((128 - exps, width), full)], axis=0),
        precision=highest, preferred_element_type=full,
    )
    for copy in loads:
        copy.wait()
    h1 = h1_in[...]
    r2 = lax.rsqrt(jnp.mean(h1 * h1, axis=1, keepdims=True) + eps_norm)

    steps = len(ys.chip_bits)
    n2_grad = router_back + n_total[...].astype(full)
    scaled = n2_grad * gains[1:2, :]
    cot_copy.wait()
    dealt = deal[at.me] - at.base
    g = dn1_send[0]
    for e in range(1, exps):
        g = jnp.where(dealt == e, dn1_send[e], g)
    hidden_grad = (
        jnp.where(valid, g.astype(full), 0.0)
        + r2 * scaled
        - h1 * (r2 * r2 * r2) * jnp.mean(scaled * h1, axis=1, keepdims=True)
    )
    dh1[...] = hidden_grad
    small_send[exps + 1 : exps + 2, :] = jnp.sum(n2_grad * h1 * r2, axis=0, keepdims=True)
    branch = hidden_grad.astype(low)
    dz_send[...] = branch
    for e in range(exps):
        total = jnp.zeros((rows, row_block), full)
        for r in range(reps):
            total = total + nt(branch[:, r * out_cols : (r + 1) * out_cols], wout[e, r])
        do_send[e] = total.astype(low)

    def do_copies():
        return [
            send(
                do_send.at[exp_peer(k)],
                do_in.at[at.exp],
                do_sem.at[SEND, exp_peer(k)],
                do_sem.at[RECV, at.exp],
                at.device(at.rep, exp_peer(k)),
            )
            for k in range(1, exps)
        ]

    for copy in do_copies():
        copy.start()
    pltpu.make_async_copy(do_send.at[at.exp], do_in.at[at.exp], do_sem.at[RECV, at.exp]).start()

    group_dz = Group(at, dz_send, dz_all, dz_sem)
    group_dz.start()
    dz_all[at.exp] = branch
    for copy in half_loads:
        copy.wait()

    def add_halves(j, _):
        y_bufs[0][j] = y_bufs[0][j] + kept[j]
        return 0

    lax.fori_loop(0, kept.shape[0], add_halves, 0)
    ys.start(0)
    n1_copy.start()

    bias_sum[...] = jnp.zeros_like(bias_sum)

    def dn1_copies():
        beside, across = turn(at.exp, 2), turn(at.exp, 1)
        return [
            functools.partial(
                send, dn1_send.at[k], dn1_in.at[j], dn1_sem.at[SEND, j], dn1_sem.at[RECV, j], at.device(at.rep, to)
            )
            for k, j, to in ((turn(at.exp, 0), 2, beside), (across, 0, across), (beside, 1, beside))
        ]

    def attend_back(i, _):
        s = turn(at.exp, i)
        @pl.when(i == 1)
        def _():
            group_dz.pass_on()

        arrived(do_in.at[s], do_sem.at[RECV, s])
        ok = lane_of((rows, rows)) < lengths[at.base + s]
        block_lane = lane_of((rows, block_cols))
        for c in range(head_cols // block_cols):
            cols = slice(c * block_cols, (c + 1) * block_cols)
            k_cols = slice(head_cols + c * block_cols, head_cols + (c + 1) * block_cols)
            v_cols = slice(2 * head_cols + c * block_cols, 2 * head_cols + (c + 1) * block_cols)
            q = qkv[s, :, cols] * scale
            k = qkv[s, :, k_cols]
            v = qkv[s, :, v_cols]
            do = do_in[s, :, cols]
            dq = jnp.zeros((rows, block_cols), full)
            dk = jnp.zeros((rows, block_cols), full)
            dv = jnp.zeros((rows, block_cols), full)
            for t in range(block_cols // head_dim):
                h = c * (block_cols // head_dim) + t
                here = jnp.logical_and(block_lane >= t * head_dim, block_lane < (t + 1) * head_dim)
                zero = jnp.zeros_like(q)
                q_h = jnp.where(here, q, zero)
                do_h = jnp.where(here, do, zero)
                scores = nt(q_h, k) + bias[h]
                p = jnp.where(ok, jnp.exp(scores - lse[s, :, h : h + 1]), 0.0)
                dp = nt(do_h, v)
                delta = jnp.sum(dp * p, axis=1, keepdims=True)
                ds = (p * (dp - delta)).astype(low)
                bias_sum[h] += ds.astype(full)
                dv = jnp.where(here, tn(p.astype(low), do), dv)
                dq = jnp.where(here, jnp.dot(ds, k, preferred_element_type=full), dq)
                dk = jnp.where(here, tn(ds, q), dk)
            dqkv[:, cols] = (dq * scale).astype(low)
            dqkv[:, k_cols] = dk.astype(low)
            dqkv[:, v_cols] = dv.astype(low)
        dqkv_t[:, pl.ds(pl.multiple_of(s * rows, rows), rows)] = dqkv[...].T
        for e in range(exps):
            dn1_send[s, :, e * row_block : (e + 1) * row_block] = jnp.dot(
                dqkv[...], wqkv[e], preferred_element_type=full
            ).astype(low)

        @pl.when(i == 0)
        def _():
            dn1_copies()[0]().start()

        @pl.when(i == 1)
        def _():
            arrived(dn1_in.at[2], dn1_sem.at[RECV, 2])
            dn1_send[s] = (dn1_send[s].astype(full) + dn1_in[2].astype(full)).astype(low)
            dn1_copies()[1]().start()

        @pl.when(i == 2)
        def _():
            dn1_copies()[2]().start()

        return 0

    lax.fori_loop(0, exps, attend_back, 0)

    n1_copy.wait()
    seg = wq_send.shape[2]
    parts = wq_send.shape[1]
    segs = mids.shape[1] - 1
    for e in range(exps):
        part = kept[0:exps, :, e * row_block : (e + 1) * row_block].reshape(exps * rows, row_block)
        total = dot(dqkv_t[...], part)
        for j in range(parts):
            wq_send[e, j] = total[j * seg : (j + 1) * seg].astype(low)

    def owner(j):
        section, within = j // (head_cols // seg), j % (head_cols // seg)
        col = section * width + at.exp * head_cols + within * seg
        block = col // seg
        return block // segs, block % segs

    def mid_place(grp, k, quad):
        return (grp * (segs + 1) + k) * QUAD + quad

    def mid_copy(src, send_sem, rep, k, e):
        dst = mids.at[rep // QUAD, k, at.quad]
        recv = mid_sem.at[mid_place(rep // QUAD, k, at.quad)]
        stays = jnp.logical_and(rep % QUAD == at.quad, e == at.exp)
        return (
            stays,
            functools.partial(send, src, dst, send_sem, recv, (at.grp, rep % QUAD, e)),
            functools.partial(pltpu.make_async_copy, src, dst, recv),
        )

    def wq_copy(i):
        e, j = i // parts, i % parts
        rep, k = owner(j)
        return mid_copy(wq_send.at[e, j], wq_sem.at[i], rep, k, e)

    def og_copy(r):
        return mid_copy(og_send.at[r], og_sem.at[r], r, segs, at.exp)

    def go(copies, act, act_local):
        stays, away, local = copies

        @pl.when(jnp.logical_not(stays))
        def _():
            act(away)

        if act_local:

            @pl.when(stays)
            def _():
                act_local(local)

    def over(count, copies, act, act_local):
        def one(i, _):
            go(copies(i), act, act_local)
            return 0

        lax.fori_loop(0, count, one, 0)

    over(exps * parts, wq_copy, lambda copy: copy().start(), lambda copy: copy().start())
    group_dz.arrive()
    grad = tn(mine[...].reshape(exps * rows, head_cols), dz_all[...].reshape(exps * rows, width))
    for r in range(reps):
        og_send[r] = grad[:, r * out_cols : (r + 1) * out_cols].T.astype(low)
    over(reps, og_copy, lambda copy: copy().start(), lambda copy: copy().start())
    homes[2].start()

    n1_grad = dn1_send[at.exp].astype(full)
    for j in range(2):
        arrived(dn1_in.at[j], dn1_sem.at[RECV, j])
        n1_grad = n1_grad + dn1_in[j].astype(full)
    x = tokens[...].astype(full)
    r1 = lax.rsqrt(jnp.mean(x * x, axis=1, keepdims=True) + eps_norm)
    scaled = n1_grad * gains[0:1, :]
    token_grad[...] = (
        dh1[...] + r1 * scaled - x * (r1 * r1 * r1) * jnp.mean(scaled * x, axis=1, keepdims=True)
    )
    small_send[exps : exps + 1, :] = jnp.sum(n1_grad * x * r1, axis=0, keepdims=True)

    router_rows = lax.dot_general(
        logit_grad, n2_in[...].astype(full), (((0,), (0,)), ((), ())), preferred_element_type=full, precision=highest
    )
    small_send[0:exps, :] = router_rows[0:exps, :]

    line_lane = lane_of((8, 128))
    line_row = row_of((8, 128))
    bias_line = jnp.zeros((8, 128), full)
    flip = jnp.where(row_of((rows, rows)) + lane_of((rows, rows)) == rows - 1, 1.0, 0.0).astype(low)
    turned_bucket = bucket_of(rows - 1 - lane_of((8, span)))
    for h in range(heads):
        high = bias_sum[h].astype(low)
        rest = (bias_sum[h] - high.astype(full)).astype(low)
        flipped = dot(high, flip) + dot(rest, flip)
        square = jnp.concatenate([flipped, jnp.zeros((rows, rows), full)], axis=1)
        turned = pltpu.roll(square, 0, 1, stride=1, stride_axis=0)
        sums = jnp.broadcast_to(jnp.sum(turned, axis=0, keepdims=True), (8, span))
        for b in range(BUCKETS):
            value = jnp.sum(jnp.where(turned_bucket == b, sums, 0.0), axis=1, keepdims=True)
            bias_line = jnp.where(jnp.logical_and(line_row == h, line_lane == b), value, bias_line)
    for h in range(heads):
        small_send[exps + 2 : exps + 3, h * 128 : (h + 1) * 128] = bias_line[h : h + 1, :]

    def small_copies():
        return [
            send(
                small_send,
                small_exp.at[at.exp],
                small_sem.at[SEND, exp_peer(k)],
                small_sem.at[RECV, at.exp],
                at.device(at.rep, exp_peer(k)),
            )
            for k in range(1, exps)
        ]

    for copy in small_copies():
        copy.start()
    small_exp[at.exp] = small_send[...]
    ys.next(0)

    def mid_sum(grp, k):
        for q in range(QUAD):
            arrived(mids.at[grp, k, q], mid_sem.at[mid_place(grp, k, q)])
        total = mids[grp, k, 0].astype(full)
        for q in range(1, QUAD):
            total = total + mids[grp, k, q].astype(full)
        return total

    far = 1 - at.grp
    for k in range(segs + 1):
        far_send[k] = mid_sum(far, k).astype(low)

    def far_copy():
        return send(far_send, far_in, far_sem.at[SEND], far_sem.at[RECV], (far, at.quad, at.exp))

    far_copy().start()
    ys.next(1)
    for k in range(1, exps):
        arrived(small_exp.at[exp_peer(k)], small_sem.at[RECV, exp_peer(k)])
    total = small_exp[0]
    for e in range(1, exps):
        total = total + small_exp[e]
    small_sum[0] = total
    for e in range(exps):
        small_sum[0, exps + 3 + e : exps + 4 + e, :] = small_exp[e, exps + 2 : exps + 3, :]

    def small2_copies():
        return [
            send(
                small_sum.at[0],
                small_rep.at[at.rep],
                small2_sem.at[SEND, (at.rep + k) % reps],
                small2_sem.at[RECV, at.rep],
                at.device((at.rep + k) % reps, at.exp),
            )
            for k in range(1, reps)
        ]

    for copy in small2_copies():
        copy.start()
    small_rep[at.rep] = small_sum[0]
    for step in range(2, steps):
        ys.next(step)
    length = lengths[at.base]
    for e in range(1, exps):
        length = jnp.where(deal[at.base + e] == at.me, lengths[at.base + e], length)
    block = ys.result()[0]
    block_out[...] = jnp.where(row_of((rows, 1)) < length, block, jnp.zeros_like(block))
    for k in range(1, reps):
        arrived(small_rep.at[(at.rep + k) % reps], small2_sem.at[RECV, (at.rep + k) % reps])
    total = small_rep[0]
    for r in range(1, reps):
        total = total + small_rep[r]
    small_out[...] = total

    near = [mid_sum(at.grp, k) for k in range(segs + 1)]
    arrived(far_in, far_sem.at[RECV])
    grads = [(near[k] + far_in[k].astype(full)).T for k in range(segs + 1)]
    qkv_grad[...] = jnp.concatenate(grads[:segs], axis=1)
    out_grad[...] = grads[segs]
    for home in homes:
        home.arrive()

    ys.finish()

    for home in homes:
        home.sent()

    over(exps * parts, wq_copy, lambda copy: copy().wait_send(), None)
    over(reps, og_copy, lambda copy: copy().wait_send(), None)
    far_copy().wait_send()
    for copies in (do_copies(), small_copies(), small2_copies()):
        for copy in copies:
            copy.wait_send()
    for copy in dn1_copies():
        copy().wait_send()
    group_dz.sent()


def routed(routes_t, seq, rows):
    pair = routes_t[:, pl.ds(pl.multiple_of(seq * rows, rows), rows)].astype(full)
    cols = jnp.concatenate([pair, jnp.zeros((126, rows), full)], axis=0).T
    lane = lane_of((rows, 128)).astype(full)
    return jnp.logical_or(lane == cols[:, 0:1], lane == cols[:, 1:2])


def backward_call(
    grps, exps, lengths, deal, bias_table, y_half, y_far, both_g, down_g, in_before, down_before, n1,
    cot_all, routes_t, tokens, n_total, c_in, n2, probs, h1, qkv, lse, mine, wqkv, wout, gains, router
):
    reps = grps * QUAD
    rows, width = tokens.shape
    heads = HEADS // exps
    head_cols = width // exps
    row_block = wqkv.shape[2]
    out_cols = wout.shape[3]
    shard_cols = 3 * width // reps
    seg = math.gcd(shard_cols, head_cols)
    segs = shard_cols // seg
    parts = 3 * head_cols // seg
    members = QUAD * exps
    chip_bits = bits_of(members) - 1
    small_rows = -(-(2 * exps + 3) // 8) * 8
    shape = jax.ShapeDtypeStruct
    vmem = pl.BlockSpec(memory_space=pltpu.VMEM)
    smem = pl.BlockSpec(memory_space=pltpu.SMEM)
    hbm = pl.BlockSpec(memory_space=pl.ANY)
    results = [
        (shape((rows, width), full), vmem),
        (shape((rows, width), low), vmem),
        (shape(in_before.shape, low), hbm),
        (shape(down_before.shape, low), hbm),
        (shape((row_block, shard_cols), full), vmem),
        (shape((row_block, out_cols), full), vmem),
        (shape((small_rows, width), full), vmem),
    ]
    dma = pltpu.SemaphoreType.DMA
    bufs = [pltpu.VMEM((1 << (chip_bits - s), rows, width), low) for s in range(chip_bits + 1)]
    return pl.pallas_call(
        functools.partial(backward_kernel, grps, exps),
        out_shape=[r[0] for r in results],
        in_specs=[smem] * 3 + [hbm] * 8 + [vmem] * 6 + [hbm] * 6 + [vmem] * 2,
        out_specs=[r[1] for r in results],
        scratch_shapes=[
            pltpu.VMEM(h1.shape, full),
            pltpu.VMEM(qkv.shape, low),
            pltpu.VMEM(lse.shape, full),
            pltpu.VMEM(mine.shape, low),
            pltpu.VMEM(wqkv.shape, low),
            pltpu.VMEM(wout.shape, low),
            pltpu.VMEM((members // 2, rows, width), low),
            list(bufs),
            pltpu.VMEM((rows, width), full),
            pltpu.VMEM((rows, width), low),
            pltpu.VMEM((exps, rows, width), low),
            pltpu.VMEM((exps, rows, head_cols), low),
            pltpu.VMEM((exps, rows, head_cols), low),
            pltpu.VMEM((heads, rows, rows), full),
            pltpu.VMEM((heads, rows, rows), full),
            pltpu.VMEM((rows, 3 * head_cols), low),
            pltpu.VMEM((3 * head_cols, exps * rows), low),
            pltpu.VMEM((exps, rows, width), low),
            pltpu.VMEM((3, rows, width), low),
            pltpu.VMEM((exps, parts, seg, row_block), low),
            pltpu.VMEM((reps, seg, row_block), low),
            pltpu.VMEM((grps, segs + 1, QUAD, seg, row_block), low),
            pltpu.VMEM((segs + 1, seg, row_block), low),
            pltpu.VMEM((segs + 1, seg, row_block), low),
            pltpu.VMEM((small_rows, width), full),
            pltpu.VMEM((exps, small_rows, width), full),
            pltpu.VMEM((1, small_rows, width), full),
            pltpu.VMEM((reps, small_rows, width), full),
            dma((2, 3 << chip_bits)),
            dma((2,)),
            dma((3, 2, 2 * reps)),
            dma((3, 2, max(QUAD, grps))),
            dma((2, exps)),
            dma((2, exps)),
            dma((2, exps)),
            dma((exps * parts,)),
            dma((reps,)),
            dma((grps * (segs + 1) * QUAD,)),
            dma((2,)),
            dma((2, exps)),
            dma((2, reps)),
            dma((2,)),
            dma((6,)),
        ],
        compiler_params=pltpu.CompilerParams(
            collective_id=1, has_side_effects=True, vmem_limit_bytes=60 * 1024 * 1024
        ),
        input_output_aliases={7: 2, 8: 3},
        name="backward",
    )(
        lengths, deal, bias_table, y_half, y_far, both_g, down_g, in_before, down_before, n1, cot_all,
        routes_t, tokens, n_total, c_in, n2, probs, h1, qkv, lse, mine, wqkv, wout, gains, router
    )


def per_device(
    tokens,
    cotangent,
    seq_lengths,
    deal,
    routes,
    attn_qkv,
    qkv_first,
    qkv_second,
    attn_out,
    out_first,
    out_second,
    rel_bias,
    bias_first,
    bias_second,
    router,
    router_first,
    router_second,
    norm_gains,
    gains_first,
    gains_second,
    expert_in,
    in_first,
    in_second,
    expert_out,
    down_first,
    down_second,
):
    rows, width = tokens.shape
    experts = router.shape[1]
    capacity = (10 * rows + 4 * experts - 1) // (4 * experts)
    exps = lax.axis_size("exp")
    grps = lax.axis_size("grp")
    routes_t = routes.T
    bias_table = rel_bias.T
    (
        both_w, down_w, cot_all, n_all, comb_all, qkv, lse, context_mine, normed_group, wqkv, wout, hidden_one,
        normed_two, router_probs, in_low, down_low,
    ) = forward_call(
        grps, exps, seq_lengths, bias_table, routes_t, tokens, cotangent, norm_gains.T, router.T,
        attn_qkv, attn_out, expert_in[0], expert_out[0],
    )
    n_total, y_half, y_far, c_in, both_g, down_g, in_before, down_before = expert_call(
        grps, exps, capacity, deal, routes_t, comb_all, n_all, cot_all, both_w, down_w, in_low, down_low,
        hidden_one,
    )
    token_grad, block_out, in_parts, down_parts, qkv_grad, out_grad, small = backward_call(
        grps, exps, seq_lengths, deal, bias_table, y_half, y_far, both_g, down_g,
        in_before, down_before, normed_group, cot_all, routes_t, tokens, n_total, c_in, normed_two, router_probs, hidden_one, qkv, lse, context_mine, wqkv,
        wout, norm_gains.T, router.T,
    )
    states = [
        attn_qkv, qkv_first, qkv_second, attn_out, out_first, out_second, bias_table, bias_first.T, bias_second.T,
        router.T, router_first.T, router_second.T, norm_gains.T, gains_first.T, gains_second.T,
        expert_in[0], in_first[0], in_second[0], expert_out[0], down_first[0], down_second[0],
    ]
    new = list(adam_call(exps, in_parts, down_parts, qkv_grad, out_grad, small, states))
    new = new[:6] + [array.T for array in new[6:15]] + [array[None] for array in new[15:]]
    return (block_out, token_grad, *new)


def bucket_onehot(length):
    places = jnp.arange(length, dtype=jnp.int32)
    offset = places[None, :] - places[:, None]
    distance = jnp.abs(offset)
    bucket = 16 * (offset > 0).astype(jnp.int32)
    for threshold in thresholds:
        bucket = bucket + (distance >= threshold).astype(jnp.int32)
    return (bucket[:, :, None] == jnp.arange(BUCKETS, dtype=jnp.int32)[None, None, :]).astype(full)


def swap(pieces, axes):
    return lax.all_to_all(pieces, axes, split_axis=0, concat_axis=0, tiled=True)


def spread(block, axes):
    members = lax.axis_size(axes)
    return swap(jnp.broadcast_to(block[None], (members,) + block.shape), axes)


def plain_device(
    tokens,
    cotangent,
    seq_lengths,
    deal,
    routes,
    attn_qkv,
    qkv_first,
    qkv_second,
    attn_out,
    out_first,
    out_second,
    rel_bias,
    bias_first,
    bias_second,
    router,
    router_first,
    router_second,
    norm_gains,
    gains_first,
    gains_second,
    expert_in,
    in_first,
    in_second,
    expert_out,
    down_first,
    down_second,
):
    rows, width = tokens.shape
    head_dim = width // HEADS
    score_scale = 1.0 / math.sqrt(head_dim)
    experts = router.shape[1]
    capacity = (10 * rows + 4 * experts - 1) // (4 * experts)
    exps = lax.axis_size("exp")
    grps = lax.axis_size("grp")
    reps = grps * QUAD
    heads = HEADS // exps
    head_cols = heads * head_dim
    place = lax.axis_index("exp")
    base = lax.axis_index(REP) * exps
    me = base + place
    slab = expert_in.shape[1]
    units = expert_out.shape[1]
    quarter = grps * units

    row_block = attn_qkv.shape[0]
    qkv_rows = lax.all_gather(attn_qkv.astype(low), REP, axis=1, tiled=True)
    out_rows = lax.all_gather(attn_out.astype(low), REP, axis=1, tiled=True)
    qkv_pieces = jnp.transpose(
        qkv_rows.reshape(row_block, 3, exps, head_cols), (2, 0, 1, 3)
    ).reshape(exps, row_block, 3 * head_cols)
    qkv_mine = swap(qkv_pieces, "exp").reshape(width, 3 * head_cols)
    full_out = spread(out_rows, "exp").reshape(width, width)

    group_tokens = spread(tokens, "exp")
    group_cotangent = spread(cotangent, "exp")
    my_cotangent = lax.dynamic_index_in_dim(group_cotangent, deal[me] - base, 0, keepdims=False)

    my_routes = lax.dynamic_slice_in_dim(routes, me * rows, rows, 0)
    places = jnp.arange(rows, dtype=jnp.int32)
    valid_rows = (places < seq_lengths[me]).astype(full)
    group_lengths = lax.dynamic_slice_in_dim(seq_lengths, base, exps, 0)
    key_ok = places[None, :] < group_lengths[:, None]
    gain_one = norm_gains[:, 0]
    gain_two = norm_gains[:, 1]

    chosen = (my_routes[:, :, None] == jnp.arange(experts, dtype=jnp.int32)[None, None, :]).astype(full)
    flat_routes = my_routes.reshape(-1)
    route_hot = (flat_routes[:, None] == jnp.arange(experts, dtype=jnp.int32)[None, :]).astype(jnp.int32)
    before = jnp.cumsum(route_hot, axis=0) - route_hot
    slot_index = jnp.sum(before * route_hot, axis=-1)
    target = (flat_routes * capacity + slot_index).reshape(rows, 2)
    slots = experts * capacity
    slot_ids = jnp.arange(slots, dtype=jnp.int32)
    place_first = slot_ids[:, None] == target[None, :, 0]
    place_second = slot_ids[:, None] == target[None, :, 1]
    place_any = jnp.logical_or(place_first, place_second).astype(low)

    shard_in = expert_in[0].astype(low).reshape(slab, 2, grps, QUAD, units)
    in_pieces = jnp.transpose(shard_in, (1, 3, 0, 2, 4)).reshape(2, 1, QUAD, slab, quarter)
    in_pieces = jnp.broadcast_to(in_pieces, (2, grps, QUAD, slab, quarter)).reshape(
        2, reps, slab, quarter
    )
    down_mine = spread(expert_out[0].astype(low), "grp").reshape(quarter, width)
    gate_mine = swap(in_pieces[0], REP).reshape(width, quarter)
    up_mine = swap(in_pieces[1], REP).reshape(width, quarter)

    upstream = my_cotangent.astype(full) * valid_rows[:, None]

    def to_experts(block):
        sent = block.reshape((1, experts) + block.shape[1:])
        sent = jnp.broadcast_to(sent, (QUAD,) + sent.shape[1:])
        return swap(sent.reshape((QUAD * experts,) + block.shape[1:]), PLANE)

    def dispatch(values):
        return dot(place_any, values).astype(low).reshape(experts, capacity, width)

    expert_upstream = to_experts(dispatch(upstream.astype(low))).reshape(-1, width)
    active_grad_bare = lax.dot_general(
        expert_upstream, down_mine, (((1,), (1,)), ((), ())), preferred_element_type=full
    )

    x_group = group_tokens.astype(full)
    scale_group = lax.rsqrt(jnp.mean(x_group * x_group, axis=-1, keepdims=True) + eps_norm)
    normed_group = (x_group * scale_group * gain_one).astype(low).reshape(exps * rows, width)
    qkv = dot(normed_group, qkv_mine).astype(low).reshape(exps, rows, 3, heads, head_dim)
    queries = qkv[:, :, 0]
    key_rows = qkv[:, :, 1]
    values = qkv[:, :, 2]
    onehot = bucket_onehot(rows)
    bias_mine = lax.dynamic_slice_in_dim(rel_bias, place * heads, heads, 1)
    bias_table = jnp.einsum("ijb,bh->hij", onehot, bias_mine, precision=highest)

    def scores_of():
        raw = (
            jnp.einsum("sihd,sjhd->shij", queries, key_rows, preferred_element_type=full)
            * score_scale
            + bias_table[None]
        )
        return jnp.where(key_ok[:, None, None, :], raw, -1e30)

    scores = scores_of()
    row_max = jnp.max(scores, axis=-1, keepdims=True)
    log_total = row_max + jnp.log(jnp.sum(jnp.exp(scores - row_max), axis=-1, keepdims=True))
    weights_low = jnp.exp(scores - log_total).astype(low)
    context_mine = (
        jnp.einsum("shij,sjhd->sihd", weights_low, values, preferred_element_type=full)
        .astype(low)
        .reshape(exps, rows, head_cols)
    )
    context = jnp.transpose(swap(context_mine, "exp"), (1, 0, 2)).reshape(rows, width)

    x_float = tokens.astype(full)
    scale_one = lax.rsqrt(jnp.mean(x_float * x_float, axis=-1, keepdims=True) + eps_norm)
    hidden_one = x_float + dot(context, full_out)
    scale_two = lax.rsqrt(jnp.mean(hidden_one * hidden_one, axis=-1, keepdims=True) + eps_norm)
    normed_two = (hidden_one * scale_two * gain_two).astype(low)
    normed_float = normed_two.astype(full)
    router_probs = jax.nn.softmax(jnp.dot(normed_float, router, precision=highest), axis=-1)
    picked = jnp.sum(router_probs[:, None, :] * chosen, axis=-1)
    gate_total = jnp.sum(picked, axis=-1, keepdims=True)
    gate_value = picked / gate_total
    combine = gate_value * valid_rows[:, None]
    combine_slots = jnp.sum(
        jnp.where(place_first, combine[None, :, 0], 0.0)
        + jnp.where(place_second, combine[None, :, 1], 0.0),
        axis=1,
    ).reshape(experts, 1, capacity)

    expert_rows = to_experts(dispatch(normed_two)).reshape(-1, width)
    expert_combine = to_experts(combine_slots).reshape(-1, 1)

    gate_part = dot(expert_rows, gate_mine)
    up_part = dot(expert_rows, up_mine)
    active_float, active_pull = jax.vjp(gated_unit, gate_part, up_part)
    active = active_float.astype(low)
    active_scaled = (active_float * expert_combine).astype(low)
    combine_grad_part = jnp.sum(active_float * active_grad_bare, axis=-1).reshape(
        QUAD * experts, 1, capacity
    )
    gate_part_grad, up_part_grad = active_pull(active_grad_bare * expert_combine)
    gate_part_grad = gate_part_grad.astype(low)
    up_part_grad = up_part_grad.astype(low)
    rows_grad_part = (
        lax.dot_general(gate_part_grad, gate_mine, (((1,), (1,)), ((), ())), preferred_element_type=full)
        + lax.dot_general(up_part_grad, up_mine, (((1,), (1,)), ((), ())), preferred_element_type=full)
    ).astype(low)
    output_part = dot(active, down_mine).astype(low)

    combine_grad_back = swap(combine_grad_part, PLANE)
    rows_grad_back = swap(rows_grad_part.reshape(QUAD * experts, capacity, width), PLANE)
    output_back = swap(output_part.reshape(QUAD * experts, capacity, width), PLANE)

    def transposed_dot(a, b):
        return lax.dot_general(a, b, (((0,), (0,)), ((), ())), preferred_element_type=full)

    down_grad = transposed_dot(active_scaled, expert_upstream).astype(low)
    gate_grad = transposed_dot(expert_rows, gate_part_grad).astype(low)
    up_grad = transposed_dot(expert_rows, up_part_grad).astype(low)
    down_share = jnp.sum(
        swap(down_grad.reshape(grps, units, width), "grp").astype(full), axis=0
    )[None]

    def in_columns(grad):
        back = swap(grad.reshape(reps, slab, quarter), REP).astype(full)
        back = jnp.sum(back.reshape(grps, QUAD, slab, grps, units), axis=0)
        return jnp.transpose(back, (1, 2, 0, 3)).reshape(slab, grps * QUAD * units)

    in_share = jnp.concatenate([in_columns(gate_grad), in_columns(up_grad)], axis=1)[None]

    def from_slots(placed, parts):
        hot = jnp.broadcast_to(placed.astype(low)[None], (QUAD,) + placed.shape).reshape(-1, rows)
        return lax.dot_general(
            hot, parts.reshape(-1, width), (((0,), (0,)), ((), ())), preferred_element_type=full
        )

    mixture = combine[:, :1] * from_slots(place_first, output_back) + combine[:, 1:] * from_slots(
        place_second, output_back
    )
    block_loader = (valid_rows[:, None] * (hidden_one + mixture)).astype(low)
    seq_ids = jnp.arange(deal.shape[0], dtype=jnp.int32)
    dealt_seq = jnp.sum(jnp.where(deal == me, seq_ids, 0))
    block_out = lax.dynamic_index_in_dim(
        spread(block_loader, "exp"), dealt_seq - base, 0, keepdims=False
    )

    combine_grad_slots = jnp.sum(combine_grad_back.reshape(QUAD, slots), axis=0)
    combine_grad = jnp.stack(
        [
            jnp.sum(jnp.where(place_first, combine_grad_slots[:, None], 0.0), axis=0),
            jnp.sum(jnp.where(place_second, combine_grad_slots[:, None], 0.0), axis=0),
        ],
        axis=1,
    )
    gate_grad_value = combine_grad * valid_rows[:, None]
    picked_grad = (
        gate_grad_value - jnp.sum(gate_grad_value * gate_value, axis=-1, keepdims=True)
    ) / gate_total
    probs_grad = jnp.sum(picked_grad[:, :, None] * chosen, axis=1)
    logit_grad = router_probs * (
        probs_grad - jnp.sum(probs_grad * router_probs, axis=-1, keepdims=True)
    )
    router_grad = jnp.dot(normed_float.T, logit_grad, precision=highest)
    normed_grad = jnp.dot(logit_grad, router.T, precision=highest) + from_slots(
        jnp.logical_or(place_first, place_second), rows_grad_back
    )
    scaled_two = normed_grad * gain_two
    hidden_grad = (
        upstream
        + scale_two * scaled_two
        - hidden_one * scale_two**3 * jnp.mean(scaled_two * hidden_one, axis=-1, keepdims=True)
    )
    gain_two_grad = jnp.sum(normed_grad * hidden_one * scale_two, axis=0)
    branch_grad = hidden_grad.astype(low)
    context_grad = lax.dot_general(
        branch_grad, full_out, (((1,), (1,)), ((), ())), preferred_element_type=full
    ).astype(low)
    context_grad_pieces = jnp.transpose(context_grad.reshape(rows, exps, head_cols), (1, 0, 2))
    context_grad_mine = swap(context_grad_pieces, "exp").reshape(exps, rows, heads, head_dim)
    branch_group = spread(branch_grad, "exp").reshape(exps * rows, width)
    out_grad = transposed_dot(context_mine.reshape(exps * rows, head_cols), branch_group).astype(low)

    scores = scores_of()
    probs_again = jnp.exp(scores - log_total)
    weights_again = probs_again.astype(low)
    values_grad = jnp.einsum(
        "shij,sihd->sjhd", weights_again, context_grad_mine, preferred_element_type=full
    )
    probs_grad_att = jnp.einsum(
        "sihd,sjhd->shij", context_grad_mine, values, preferred_element_type=full
    )
    row_delta = jnp.sum(probs_grad_att * probs_again, axis=-1, keepdims=True)
    scores_grad = (probs_again * (probs_grad_att - row_delta)).astype(low)
    scores_grad_sum = jnp.sum(scores_grad.astype(full), axis=0)
    bias_grad_mine = jnp.einsum("hij,ijb->bh", scores_grad_sum, onehot, precision=highest)
    bias_grad = lax.dynamic_update_slice_in_dim(
        jnp.zeros((BUCKETS, HEADS), full), bias_grad_mine, place * heads, 1
    )
    queries_grad = (
        jnp.einsum("shij,sjhd->sihd", scores_grad, key_rows, preferred_element_type=full)
        * score_scale
    )
    keys_grad = (
        jnp.einsum("shij,sihd->sjhd", scores_grad, queries, preferred_element_type=full)
        * score_scale
    )
    qkv_grad = (
        jnp.stack([queries_grad, keys_grad, values_grad], axis=2)
        .astype(low)
        .reshape(exps * rows, 3 * head_cols)
    )
    normed_one_part = lax.dot_general(
        qkv_grad, qkv_mine, (((1,), (1,)), ((), ())), preferred_element_type=full
    ).astype(low)
    normed_one_grad = jnp.sum(
        swap(normed_one_part.reshape(exps, rows, width), "exp").astype(full), axis=0
    )
    scaled_one = normed_one_grad * gain_one
    token_grad = (
        hidden_grad
        + scale_one * scaled_one
        - x_float * scale_one**3 * jnp.mean(scaled_one * x_float, axis=-1, keepdims=True)
    )
    gain_one_grad = jnp.sum(normed_one_grad * x_float * scale_one, axis=0)

    qkv_weight_grad = transposed_dot(normed_group, qkv_grad).astype(low)
    qkv_grad_rows = swap(qkv_weight_grad.reshape(exps, row_block, 3 * head_cols), "exp")
    qkv_grad_rows = jnp.transpose(
        qkv_grad_rows.reshape(exps, row_block, 3, head_cols), (1, 2, 0, 3)
    ).reshape(row_block, reps, -1)
    qkv_share = jnp.sum(
        swap(jnp.transpose(qkv_grad_rows, (1, 0, 2)), REP).astype(full), axis=0
    )
    out_pieces = jnp.transpose(out_grad.reshape(row_block, reps, -1), (1, 0, 2))
    out_share = jnp.sum(swap(out_pieces, REP).astype(full), axis=0)

    small = jnp.concatenate(
        [
            router_grad.reshape(-1),
            jnp.stack([gain_one_grad, gain_two_grad], axis=1).reshape(-1),
            bias_grad.reshape(-1),
        ]
    ).reshape(-1, 128)
    small_total = jnp.sum(lax.all_gather(small, ALL, axis=0, tiled=False), axis=0).reshape(-1)
    router_total = small_total[: router.size].reshape(router.shape)
    gains_total = small_total[router.size : router.size + norm_gains.size].reshape(norm_gains.shape)
    bias_total = small_total[router.size + norm_gains.size :].reshape(rel_bias.shape)

    qkv_new = adamw_update(attn_qkv, qkv_first, qkv_second, qkv_share, 1.5 / math.sqrt(D), 0.1)
    out_new = adamw_update(attn_out, out_first, out_second, out_share, 6.0 / math.sqrt(D), 0.1)
    bias_new = adamw_update(rel_bias, bias_first, bias_second, bias_total, 0.3, 0.0)
    router_new = adamw_update(
        router, router_first, router_second, router_total, 1.0 / math.sqrt(D), 0.1
    )
    gains_new = adamw_update(norm_gains, gains_first, gains_second, gains_total, 0.5, 0.0)
    in_new = adamw_update(expert_in, in_first, in_second, in_share, 1.5 / math.sqrt(D), 0.1)
    down_new = adamw_update(
        expert_out, down_first, down_second, down_share, 1.5 / math.sqrt(FF), 0.1
    )
    return (
        (block_out, token_grad)
        + qkv_new
        + out_new
        + bias_new
        + router_new
        + gains_new
        + in_new
        + down_new
    )


def solution(mesh):
    reps, exps = mesh.devices.shape
    split = Mesh(mesh.devices.reshape(reps // QUAD, QUAD, exps), ALL)
    by_rows = P(ALL, None)
    attn = P("exp", REP)
    expert = P("exp", REP, None)
    return jax.shard_map(
        per_device if (reps, exps) == (2 * QUAD, 4) else plain_device,
        mesh=split,
        in_specs=(by_rows, by_rows) + (P(),) * 3 + (attn,) * 6 + (P(),) * 9 + (expert,) * 6,
        out_specs=(by_rows, by_rows) + (attn,) * 6 + (P(),) * 9 + (expert,) * 6,
        check_vma=False,
    )
```

```python
import functools
import math

import jax
import jax.numpy as jnp
from jax import lax
from jax.experimental import pallas as pl
from jax.experimental.pallas import tpu as pltpu
from jax.sharding import Mesh
from jax.sharding import PartitionSpec as P

D = 1024
HEADS = 16
FF = 2816
BUCKETS = 32
STEP = 10
QUAD = 4
REP = ("grp", "quad")
PLANE = ("quad", "exp")
ALL = ("grp", "quad", "exp")

highest = lax.Precision.HIGHEST
eps_norm = 1e-06
thresholds = (1, 2, 3, 4, 5, 6, 7, 8, 11, 16, 22, 32, 45, 64, 90)
beta_one = 0.9
beta_two = 0.999
eps_adam = 1e-08
low = jnp.bfloat16
full = jnp.float32
MESH = pl.DeviceIdType.MESH


def adamw_update(weight, moment, second, gradient, step_rate, decay_factor):
    new_moment = beta_one * moment + (1.0 - beta_one) * gradient
    new_second = beta_two * second + (1.0 - beta_two) * gradient * gradient
    corrected = new_moment / (1.0 - beta_one**STEP)
    scaled = new_second / (1.0 - beta_two**STEP)
    new_weight = weight - step_rate * (
        corrected / (jnp.sqrt(scaled) + eps_adam) + decay_factor * weight
    )
    return (new_moment, new_second, new_weight)


def gated_unit(gate_input, up_input):
    return jax.nn.gelu(gate_input, approximate=True) * up_input


def dot(a, b):
    return jnp.dot(a, b, preferred_element_type=full)


def nt(a, b, precision=None):
    return lax.dot_general(a, b, (((1,), (1,)), ((), ())), preferred_element_type=full, precision=precision)


def tn(a, b):
    return lax.dot_general(a, b, (((0,), (0,)), ((), ())), preferred_element_type=full)


class Where:
    def __init__(self, grps, exps):
        self.grps, self.exps = grps, exps
        self.reps = grps * QUAD
        self.grp = lax.axis_index("grp")
        self.quad = lax.axis_index("quad")
        self.exp = lax.axis_index("exp")
        self.rep = self.grp * QUAD + self.quad
        self.base = self.rep * exps
        self.me = self.base + self.exp

    def device(self, rep, exp):
        return (rep // QUAD, rep % QUAD, exp)

    def near(self, flip):
        q = self.quad
        if flip & 1:
            q = q + 1 - 2 * (q % 2)
        if flip & 2:
            q = q + 2 - 4 * (q // 2)
        return q


def send(src, dst, send_sem, recv_sem, device):
    return pltpu.make_async_remote_copy(
        src_ref=src, dst_ref=dst, send_sem=send_sem, recv_sem=recv_sem, device_id=device, device_id_type=MESH
    )


def arrived(ref, sem):
    pltpu.make_async_copy(ref, ref, sem).wait()


def greet(count, device):
    barrier = pltpu.get_barrier_semaphore()

    def one(k, _):
        pl.semaphore_signal(barrier, inc=1, device_id=device(k), device_id_type=MESH)
        return 0

    lax.fori_loop(1, count + 1, one, 0)
    return functools.partial(pl.semaphore_wait, barrier, count)


def everyone(at):
    count = at.reps * at.exps

    def device(k):
        other = (at.me + k) % count
        return at.device(other // at.exps, other % at.exps)

    return count - 1, device


def neighbours(at):
    members = QUAD * at.exps
    plane = at.quad * at.exps + at.exp

    def device(k):
        other = (plane + k) % members
        rest = k - members
        grp = jnp.where(k < members, at.grp, (at.grp + 1 + rest // QUAD) % at.grps)
        quad = jnp.where(k < members, other // at.exps, rest % QUAD)
        return grp, quad, jnp.where(k < members, other % at.exps, at.exp)

    return members - 1 + QUAD * (at.grps - 1), device


def turn(exp, i):
    beside = exp + 1 - 2 * (exp % 2)
    return jnp.where(i == 0, (beside + 2) % 4, jnp.where(i == 1, (exp + 2) % 4, jnp.where(i == 2, beside, exp)))


def lane_of(shape):
    return lax.broadcasted_iota(jnp.int32, shape, 1)


def row_of(shape):
    return lax.broadcasted_iota(jnp.int32, shape, 0)


def bucket_of(offset):
    distance = jnp.abs(offset)
    bucket = jnp.where(offset > 0, 16, 0)
    for threshold in thresholds:
        bucket = bucket + jnp.where(distance >= threshold, 1, 0)
    return bucket


def bits_of(count):
    return count.bit_length() - 1


def column_parts(width):
    tiles = width // 128
    cuts = [0, (tiles + 2) // 3, (2 * tiles + 2) // 3, tiles]
    return [(cuts[i] * 128, (cuts[i + 1] - cuts[i]) * 128) for i in range(3)]


def flipped(place, bit):
    return place + (1 - 2 * ((place // (1 << bit)) % 2)) * (1 << bit)


class Doubling:
    def __init__(self, at, own, every, sems, core_sems, orders):
        self.at, self.own, self.every = at, own, every
        self.sems, self.core_sems, self.orders = sems, core_sems, orders
        self.plane = at.quad * at.exps + at.exp
        self.steps = len(orders[0])
        self.parts = column_parts(own.shape[1])

    def device(self, bit):
        other = flipped(self.plane, bit)
        return (self.at.grp, other // self.at.exps, other % self.at.exps)

    def place(self, part, j):
        p = self.plane
        for i, bit in enumerate(self.orders[part]):
            if (j >> i) & 1:
                p = flipped(p, bit + 1)
        return p

    def block(self, part, p):
        begin, size = self.parts[part]
        return self.every.at[p, :, pl.ds(begin, size)]

    def source(self, part, j):
        begin, size = self.parts[part]
        return self.own.at[:, pl.ds(begin, size)] if j == 0 else self.block(part, self.place(part, j))

    def index(self, step, part, j):
        return part * (1 << self.steps) + (1 << step) - 1 + j

    def copy(self, step, part, j):
        i = self.index(step, part, j)
        return send(
            self.source(part, j),
            self.block(part, self.place(part, j)),
            self.sems.at[0, i],
            self.sems.at[1, i],
            self.device(self.orders[part][step] + 1),
        )

    def core_copy(self, part, j):
        i = part * (1 << self.steps) + j
        return send(
            self.source(part, j),
            self.block(part, self.place(part, j)),
            self.core_sems.at[0, i],
            self.core_sems.at[1, i],
            self.device(0),
        )

    def start(self):
        for part in range(3):
            for step in range(self.steps):
                self.copy(step, part, 0).start()
        for part in range(3):
            self.core_copy(part, 0).start()
        self.keep().start()

    def keep(self):
        return pltpu.make_async_copy(self.own, self.every.at[self.plane], self.core_sems.at[1, 3 << self.steps])

    def next(self, step):
        for part in range(3):
            for j in range(1 << step):
                k = (1 << step) + j
                arrived(self.block(part, self.place(part, k)), self.sems.at[1, self.index(step, part, j)])
                for later in range(step + 1, self.steps):
                    self.copy(later, part, k).start()
                self.core_copy(part, k).start()

    def finish_in(self):
        for part in range(3):
            for j in range(1 << self.steps):
                there = self.block(part, flipped(self.place(part, j), 0))
                arrived(there, self.core_sems.at[1, part * (1 << self.steps) + j])
        self.keep().wait()

    def finish_out(self):
        for part in range(3):
            for j in range(1 << self.steps):
                self.core_copy(part, j).wait_send()
            for step in range(self.steps):
                for j in range(1 << step):
                    self.copy(step, part, j).wait_send()


class Halving:
    def __init__(self, at, bufs, sems, orders):
        self.at, self.bufs, self.sems = at, bufs, sems
        self.plane = at.quad * at.exps + at.exp
        self.places = bits_of(QUAD * at.exps)
        self.chip_bits = list(range(self.places - 1))
        self.parts = column_parts(bufs[0].shape[2])
        self.orders = orders

    def device(self, bit):
        other = flipped(self.plane, bit)
        return (self.at.grp, other // self.at.exps, other % self.at.exps)

    def hop(self, step, part):
        order = self.orders[part]
        bit = order[step]
        left = [b for b in self.chip_bits if b not in order[:step]]
        pos = left.index(bit)
        half = 1 << (len(left) - 1)
        mine = (self.plane // (1 << (bit + 1))) % 2
        device = self.device(bit + 1)
        begin, size = self.parts[part]
        cols = pl.ds(begin, size)
        base = self.base(step, part)

        def index(j, value):
            return (j >> pos) * (1 << (pos + 1)) + value * (1 << pos) + j % (1 << pos)

        pairs = []
        for j in range(half):
            copy = functools.partial(
                send,
                self.bufs[step].at[index(j, 1 - mine), :, cols],
                self.bufs[step + 1].at[j, :, cols],
                self.sems.at[0, base + j],
                self.sems.at[1, base + j],
                device,
            )
            pairs.append((copy, index(j, mine), j))
        return pairs, begin, size, base

    def base(self, step, part):
        n = len(self.chip_bits)
        return part * (1 << n) + sum(1 << (n - 1 - s) for s in range(step))

    def start(self, step, part=None):
        for p in range(3) if part is None else [part]:
            for copy, _, _ in self.hop(step, p)[0]:
                copy().start()

    def add(self, step, part):
        pairs, begin, size, base = self.hop(step, part)
        cols = pl.ds(begin, size)
        here, there = self.bufs[step], self.bufs[step + 1]
        for _, keep, j in pairs:
            arrived(there.at[j, :, cols], self.sems.at[1, base + j])
            there[j, :, begin : begin + size] = (
                there[j, :, begin : begin + size] + here[keep, :, begin : begin + size]
            )

    def next(self, step):
        for p in range(3):
            self.add(step, p)
            if step + 1 < len(self.chip_bits):
                self.start(step + 1, p)

    def result(self):
        return self.bufs[len(self.chip_bits)]

    def finish(self):
        for step in range(len(self.chip_bits)):
            for p in range(3):
                for copy, _, _ in self.hop(step, p)[0]:
                    copy().wait_send()


class Group:
    def __init__(self, at, own, every, sems):
        self.at, self.own, self.every, self.sems = at, own, every, sems
        self.beside, self.across = at.exp + 1 - 2 * (at.exp % 2), (at.exp + 2) % 4

    def copy(self, src, index, send_index, device):
        return send(
            src, self.every.at[index], self.sems.at[0, send_index], self.sems.at[1, index], self.at.device(self.at.rep, device)
        )

    def first(self):
        return [
            self.copy(self.own, self.at.exp, 0, self.across),
            self.copy(self.own, self.at.exp, 1, self.beside),
        ]

    def second(self):
        return self.copy(self.every.at[self.across], self.across, 2, self.beside)

    def start(self):
        for copy in self.first():
            copy.start()

    def pass_on(self):
        arrived(self.every.at[self.across], self.sems.at[1, self.across])
        self.second().start()

    def arrive(self):
        for index in (self.beside, (self.beside + 2) % 4):
            arrived(self.every.at[index], self.sems.at[1, index])

    def sent(self):
        for copy in self.first() + [self.second()]:
            copy.wait_send()


class Tiles:
    def __init__(self, units, reps):
        self.units = units
        self.reps = reps
        self.hidden = units * reps
        self.half = self.hidden // 256
        self.wide = (self.half + 1) // 2
        self.count = 3
        self.size = 128 * self.wide // self.count
        self.skip = 128 * (2 * self.wide - self.half)

    def start(self, quad):
        return 128 * (self.half * (quad // 2) + (self.half - self.wide) * (quad % 2))

    def rows(self, tile):
        result = []
        for k in range(QUAD):
            found = None
            for parity in range(2):
                first = self.start(parity) + tile * self.size
                live = first + (self.skip if parity and tile == 0 else 0)
                begin = max(live, k * self.units)
                end = min(first + self.size, (k + 1) * self.units)
                if end > begin:
                    found = (begin - k * self.units, end - begin, parity, begin - first)
            result.append(found)
        return result


class Outward:
    def __init__(self, at, tiles, tile, in_low, down_slab, both_w, down_w, nothing, sems, down_sems):
        self.at, self.tiles, self.tile = at, tiles, tile
        self.in_low, self.down_slab, self.both_w, self.down_w = in_low, down_slab, both_w, down_w
        self.nothing, self.sems, self.down_sems = nothing, sems, down_sems
        self.slab = in_low.shape[0]

    def source(self, quad, section):
        begin = section * self.tiles.hidden + self.tiles.start(quad) + self.tile * self.tiles.size
        return self.in_low.at[:, pl.ds(pl.multiple_of(begin, 128), self.tiles.size)]

    def target(self, rep, section):
        rows = pl.ds(pl.multiple_of(rep * self.slab, self.slab), self.slab)
        return self.both_w.at[rows, pl.ds(section * self.tiles.size, self.tiles.size)]

    def over(self, act):
        at = self.at

        def one(k, _):
            other = (at.rep + k) % at.reps
            for section in range(2):
                act(
                    functools.partial(
                        send,
                        self.source(other % QUAD, section),
                        self.target(at.rep, section),
                        self.sems.at[0, section * at.reps + other],
                        self.sems.at[1, section * at.reps + at.rep],
                        at.device(other, at.exp),
                    )
                )
            return 0

        lax.fori_loop(1, at.reps, one, 0)

    def over_down(self, act, act_local):
        at = self.at
        for k, piece in enumerate(self.tiles.rows(self.tile)):
            if piece is None:
                continue
            begin, count, parity, to = piece
            quad = 2 * (at.rep // QUAD) + parity
            src, dst = self.down_slab.at[pl.ds(begin, count)], self.down_w.at[pl.ds(to, count)]
            recv = self.down_sems.at[1, at.rep]
            for g in range(at.grps):
                stays = jnp.logical_and(at.grp == g, at.quad == quad)
                ours = at.rep % QUAD == k

                @pl.when(jnp.logical_and(ours, jnp.logical_not(stays)))
                def _():
                    act(functools.partial(send, src, dst, self.down_sems.at[0, g], recv, (g, quad, at.exp)))

                @pl.when(jnp.logical_and(ours, stays))
                def _():
                    act_local(functools.partial(pltpu.make_async_copy, src, dst, recv))

    def blank(self):
        return pltpu.make_async_copy(
            self.nothing, self.down_w.at[pl.ds(0, self.tiles.skip)], self.down_sems.at[1, self.at.reps]
        )

    def start(self):
        at = self.at
        self.over_down(lambda copy: copy().start(), lambda copy: copy().start())
        self.over(lambda copy: copy().start())
        for section in range(2):
            pltpu.make_async_copy(
                self.source(at.quad, section), self.target(at.rep, section), self.sems.at[1, section * at.reps + at.rep]
            ).start()
        if self.tile == 0:

            @pl.when(at.quad % 2 == 1)
            def _():
                self.blank().start()

    def arrive(self):
        at = self.at

        def one(rep, _):
            for section in range(2):
                arrived(self.target(rep, section), self.sems.at[1, section * at.reps + rep])
            return 0

        lax.fori_loop(0, at.reps, one, 0)
        for parity in range(2):

            @pl.when(at.quad % 2 == parity)
            def _():
                for k, piece in enumerate(self.tiles.rows(self.tile)):
                    if piece is not None and piece[2] == parity:
                        source = QUAD * (at.quad // 2) + k
                        arrived(self.down_w.at[pl.ds(piece[3], piece[1])], self.down_sems.at[1, source])
                if parity and self.tile == 0:
                    self.blank().wait()

    def sent(self):
        self.over(lambda copy: copy().wait_send())
        self.over_down(lambda copy: copy().wait_send(), lambda copy: None)


class Homeward:
    def __init__(self, at, tiles, tile, both, down, in_parts, down_parts, sems, down_sems, sections=(0, 1)):
        self.at, self.tiles, self.tile, self.sections = at, tiles, tile, sections
        self.both, self.down, self.in_parts, self.down_parts = both, down, in_parts, down_parts
        self.sems, self.down_sems = sems, down_sems
        self.slab = in_parts.shape[1]

    def target(self, grp, quad, parity, section):
        skip = self.tiles.skip if parity and self.tile == 0 else 0
        to = section * self.tiles.hidden + self.tiles.start(quad) + self.tile * self.tiles.size + skip
        to = to if isinstance(to, int) else pl.multiple_of(to, 128)
        return skip, self.in_parts.at[grp, :, pl.ds(to, self.tiles.size - skip)]

    def copy(self, rep, parity, section, local=False):
        at = self.at
        skip, dst = self.target(at.grp, at.quad, parity, section)
        rows = pl.ds(pl.multiple_of(rep * self.slab, self.slab), self.slab)
        src = self.both.at[rows, pl.ds(section * self.tiles.size + skip, self.tiles.size - skip)]
        recv = self.sems.at[1, section * at.reps + at.rep]
        if local:
            return pltpu.make_async_copy(src, dst, recv)
        return send(src, dst, self.sems.at[0, section * at.reps + rep], recv, at.device(rep, at.exp))

    def over(self, act, act_local):
        at = self.at
        for parity in range(2):

            @pl.when(at.quad % 2 == parity)
            def _():
                def one(k, _):
                    for section in self.sections:
                        act(self.copy((at.rep + k) % at.reps, parity, section))
                    return 0

                lax.fori_loop(1, at.reps, one, 0)
                if act_local:
                    for section in self.sections:
                        act_local(self.copy(at.rep, parity, section, local=True))

    def over_down(self, act, act_local):
        at = self.at
        if self.down is None:
            return
        for k, piece in enumerate(self.tiles.rows(self.tile)):
            if piece is None:
                continue
            begin, count, parity, to = piece
            src, dst = self.down.at[pl.ds(to, count)], self.down_parts.at[at.grp, pl.ds(begin, count)]
            recv = self.down_sems.at[1, at.grp]
            stays = jnp.logical_and(at.grp == at.quad // 2, at.quad == k)
            ours = at.quad % 2 == parity

            @pl.when(jnp.logical_and(ours, jnp.logical_not(stays)))
            def _():
                act(functools.partial(send, src, dst, self.down_sems.at[0, k], recv, (at.quad // 2, k, at.exp)))

            @pl.when(jnp.logical_and(ours, stays))
            def _():
                act_local(functools.partial(pltpu.make_async_copy, src, dst, recv))

    def start(self):
        self.over_down(lambda copy: copy().start(), lambda copy: copy().start())
        self.over(lambda copy: copy.start(), lambda copy: copy.start())

    def arrive(self):
        at = self.at
        for rep in range(at.reps):
            for section in self.sections:
                _, dst = self.target(rep // QUAD, rep % QUAD, rep % 2, section)
                arrived(dst, self.sems.at[1, section * at.reps + rep])
        for k, piece in enumerate(self.tiles.rows(self.tile)):
            if piece is None or self.down is None:
                continue

            @pl.when(at.quad == k)
            def _():
                for g in range(at.grps):
                    arrived(self.down_parts.at[g, pl.ds(piece[0], piece[1])], self.down_sems.at[1, g])

    def sent(self):
        self.over(lambda copy: copy.wait_send(), None)
        self.over_down(lambda copy: copy().wait_send(), lambda copy: None)


def forward_kernel(
    grps,
    exps,
    lengths,
    bias_table,
    routes_t,
    tokens,
    cotangent,
    gains,
    router,
    attn_qkv,
    attn_out,
    expert_in,
    expert_out,
    both_w,
    down_w,
    cot_all,
    n_all,
    comb_all,
    qkv_out,
    lse_out,
    mine_out,
    n1_out,
    wqkv_out,
    wout_out,
    h1_out,
    n2_out,
    probs_out,
    in_out,
    down_out,
    in_wide,
    down_wide,
    qkv_t,
    out_w,
    in_low,
    down_slab,
    tok_all,
    wqkv,
    wout,
    n1,
    qkv,
    lse,
    mine,
    ctx,
    bias,
    comb_send,
    nothing,
    tok_sem,
    wq_sem,
    wo_sem,
    wo2_sem,
    weight_sem,
    down_sem,
    ctx_sem,
    cot_sem,
    cot_core_sem,
    n_sem,
    n_core_sem,
    comb_sem,
    store_sem,
    cast_sem,
):
    at = Where(grps, exps)
    reps = at.reps
    rows, width = tokens.shape
    heads = HEADS // exps
    head_dim = width // HEADS
    head_cols = heads * head_dim
    block_cols = min(128, head_cols)
    shard_cols, row_block = qkv_t.shape
    seg = math.gcd(shard_cols, head_cols)
    segs = shard_cols // seg
    tiles = Tiles(down_slab.shape[0], reps)
    plane = at.quad * exps + at.exp
    members = QUAD * exps
    scale = 1.0 / math.sqrt(head_dim)
    SEND, RECV = 0, 1

    met = greet(*everyone(at))
    wide_copies = [
        pltpu.make_async_copy(expert_in, in_wide, cast_sem.at[0]),
        pltpu.make_async_copy(expert_out, down_wide, cast_sem.at[1]),
    ]
    for copy in wide_copies:
        copy.start()
    qkv_t[...] = attn_qkv[...].T.astype(low)
    out_w[...] = attn_out[...].astype(low)
    met()

    def exp_peer(k):
        return (at.exp + k) % exps

    group_tokens = Group(at, tokens, tok_all, tok_sem)
    group_tokens.start()
    tok_all[at.exp] = tokens[...]

    def segment(k):
        col = (at.rep * segs + k) * seg
        section = col // width
        within = col - section * width
        owner = within // head_cols
        return owner, section * head_cols + within - owner * head_cols

    def segment_copy(k, shift):
        owner, offset = segment(k)
        src = qkv_t.at[pl.ds(k * seg, seg)]
        dst = wqkv.at[at.exp, pl.ds(pl.multiple_of(offset, seg), seg)]
        target = at.device((at.rep + shift) % reps, owner)
        return owner, src, dst, functools.partial(
            send, src, dst, wq_sem.at[SEND, k * reps + shift], wq_sem.at[RECV, at.exp * 3 * (head_cols // seg) + offset // seg], target
        )

    def over_segments(act, act_local):
        def one(i, _):
            k, shift = i // reps, i % reps
            owner, src, dst, copy = segment_copy(k, shift)
            stays = jnp.logical_and(shift == 0, owner == at.exp)

            @pl.when(jnp.logical_not(stays))
            def _():
                act(copy())

            @pl.when(stays)
            def _():
                act_local(k, src, dst)

            return 0

        lax.fori_loop(0, segs * reps, one, 0)

    def local_segment(k, src, dst):
        _, offset = segment(k)
        pltpu.make_async_copy(src, dst, wq_sem.at[RECV, at.exp * 3 * (head_cols // seg) + offset // seg]).start()

    over_segments(lambda copy: copy.start(), local_segment)

    for k in range(1, reps):
        other = (at.rep + k) % reps
        send(
            out_w, wout.at[at.exp, at.rep], wo_sem.at[SEND, other], wo_sem.at[RECV, at.rep], at.device(other, at.exp)
        ).start()
    wout[at.exp, at.rep] = out_w[...]
    chip_bits = list(range(bits_of(members) - 1))
    cots = Doubling(at, cotangent, cot_all, cot_sem, cot_core_sem, [chip_bits[::-1]] * 3)
    cots.start()

    span = 2 * rows
    bucket = bucket_of(lane_of((8, span)) - rows)
    for h in range(heads):
        line = jnp.zeros((8, span), full)
        for b in range(BUCKETS):
            line = jnp.where(bucket == b, bias_table[at.exp * heads + h, b], line)
        whole = jnp.broadcast_to(line[0:1], (rows, span))
        bias[h] = pltpu.roll(whole, 0, 1, stride=1, stride_axis=0)[:, rows:]

    group_tokens.pass_on()
    group_tokens.arrive()

    def norm_group(s, _):
        x = tok_all[s].astype(full)
        r = lax.rsqrt(jnp.mean(x * x, axis=1, keepdims=True) + eps_norm)
        n1[s] = (x * r * gains[0:1, :]).astype(low)
        return 0

    lax.fori_loop(0, exps, norm_group, 0)

    for copy in wide_copies:
        copy.wait()
    in_low[...] = in_wide[...].astype(low)
    down_slab[...] = down_wide[...].astype(low)
    nothing[...] = jnp.zeros_like(nothing)
    weights = [
        Outward(
            at, tiles, t, in_low, down_slab, both_w.at[t], down_w.at[t], nothing, weight_sem.at[t], down_sem.at[t]
        )
        for t in range(2)
    ]
    weights[0].start()

    def wait_segment(i, _):
        e, j = i // (3 * head_cols // seg), i % (3 * head_cols // seg)
        arrived(wqkv.at[e, pl.ds(pl.multiple_of(j * seg, seg), seg)], wq_sem.at[RECV, i])
        return 0

    lax.fori_loop(0, exps * 3 * head_cols // seg, wait_segment, 0)

    def project(s, _):
        total = jnp.zeros((rows, 3 * head_cols), full)
        for e in range(exps):
            total = total + nt(n1[s, :, e * row_block : (e + 1) * row_block], wqkv[e])
        qkv[s] = total.astype(low)
        return 0

    lax.fori_loop(0, exps, project, 0)

    group_wout = Group(at, wout.at[at.exp], wout, wo2_sem)

    def beside(k):
        if k == 1:
            for j in range(1, reps):
                other = (at.rep + j) % reps
                arrived(wout.at[at.exp, other], wo_sem.at[RECV, other])
            group_wout.start()
        elif k == 2:
            cots.next(0)
        else:
            group_wout.pass_on()

    def attend(i, _):
        s = turn(at.exp, i)
        for k in range(1, exps):

            @pl.when(i == k)
            def _():
                beside(k)

        ok = lane_of((rows, rows)) < lengths[at.base + s]
        lane = lane_of((rows, block_cols))
        sums = jnp.zeros((rows, 128), full)
        for c in range(head_cols // block_cols):
            cols = slice(c * block_cols, (c + 1) * block_cols)
            q = qkv[s, :, cols] * scale
            k = qkv[s, :, head_cols + c * block_cols : head_cols + (c + 1) * block_cols]
            v = qkv[s, :, 2 * head_cols + c * block_cols : 2 * head_cols + (c + 1) * block_cols]
            result = jnp.zeros((rows, block_cols), full)
            for t in range(block_cols // head_dim):
                h = c * (block_cols // head_dim) + t
                here = jnp.logical_and(lane >= t * head_dim, lane < (t + 1) * head_dim)
                scores = nt(jnp.where(here, q, jnp.zeros_like(q)), k) + bias[h]
                scores = jnp.where(ok, scores, -1e30)
                top = jnp.max(scores, axis=1, keepdims=True)
                weights = jnp.exp(scores - top)
                total = jnp.sum(weights, axis=1, keepdims=True)
                weights = (weights * (1.0 / total)).astype(low)
                result = jnp.where(here, jnp.dot(weights, v, preferred_element_type=full), result)
                sums = jnp.where(lane_of((rows, 128)) == h, top + jnp.log(total), sums)
            mine[s, :, cols] = result.astype(low)
        lse[s] = sums

        @pl.when(i < exps - 1)
        def _():
            send(
                mine.at[s], ctx.at[at.exp], ctx_sem.at[SEND, s], ctx_sem.at[RECV, at.exp], at.device(at.rep, s)
            ).start()

        @pl.when(i == exps - 1)
        def _():
            pltpu.make_async_copy(mine.at[s], ctx.at[at.exp], ctx_sem.at[RECV, at.exp]).start()

        return 0

    lax.fori_loop(0, exps, attend, 0)

    cots.next(1)
    group_wout.arrive()
    for e in range(exps):
        arrived(ctx.at[e], ctx_sem.at[RECV, e])

    out_cols = wout.shape[3]
    for r in range(reps):
        cols = slice(r * out_cols, (r + 1) * out_cols)
        total = tokens[:, cols].astype(full)
        for e in range(exps):
            total = total + jnp.dot(ctx[e], wout[e, r], preferred_element_type=full)
        h1_out[:, cols] = total
    h1 = h1_out[...]
    r2 = lax.rsqrt(jnp.mean(h1 * h1, axis=1, keepdims=True) + eps_norm)
    n2 = (h1 * r2 * gains[1:2, :]).astype(low)
    n2_out[...] = n2
    rotated = [chip_bits[c:] + chip_bits[:c] for c in range(3)]
    rows_two = Doubling(at, n2_out, n_all, n_sem, n_core_sem, rotated)
    rows_two.start()
    weights[1].start()

    router_rows = jnp.concatenate([router[...], jnp.zeros((128 - exps, width), full)], axis=0)
    logits = nt(n2.astype(full), router_rows, precision=highest)
    lane = lane_of((rows, 128))
    logits = jnp.where(lane < exps, logits, -1e30)
    probs = jnp.exp(logits - jnp.max(logits, axis=1, keepdims=True))
    probs = probs / jnp.sum(probs, axis=1, keepdims=True)
    probs_out[...] = probs
    picked = jnp.where(routed(routes_t, at.me, rows), probs, 0.0)
    comb = picked / jnp.sum(picked, axis=1, keepdims=True)
    comb = jnp.where(row_of((rows, 1)) < lengths[at.me], comb, 0.0)
    comb_send[...] = comb.T[0 : comb_send.shape[0]]

    def comb_copy(k):
        other = (plane + k) % members
        return send(
            comb_send,
            comb_all.at[plane],
            comb_sem.at[SEND, other],
            comb_sem.at[RECV, plane],
            (at.grp, other // exps, other % exps),
        )

    def start_comb(k, _):
        comb_copy(k).start()
        return 0

    lax.fori_loop(1, members, start_comb, 0)
    pltpu.make_async_copy(comb_send, comb_all.at[plane], comb_sem.at[RECV, plane]).start()
    rows_two.next(0)

    stores = [
        (qkv, qkv_out),
        (lse, lse_out),
        (mine, mine_out),
        (n1, n1_out),
        (wqkv, wqkv_out),
        (wout, wout_out),
        (in_low, in_out),
        (down_slab, down_out),
    ]
    for i, (src, dst) in enumerate(stores):
        pltpu.make_async_copy(src, dst, store_sem.at[i]).start()

    for step in range(1, rows_two.steps):
        rows_two.next(step)
    for step in range(2, cots.steps):
        cots.next(step)

    cots.finish_in()
    rows_two.finish_in()

    def comb_in(k, _):
        arrived(comb_all.at[k], comb_sem.at[RECV, k])
        return 0

    lax.fori_loop(0, members, comb_in, 0)
    for tile in weights:
        tile.arrive()

    for k in range(1, exps):
        peer = exp_peer(k)
        arrived(mine.at[peer], ctx_sem.at[SEND, peer])
    over_segments(lambda copy: copy.wait_send(), lambda k, src, dst: None)
    for k in range(1, reps):
        arrived(out_w, wo_sem.at[SEND, (at.rep + k) % reps])
    group_tokens.sent()
    group_wout.sent()
    cots.finish_out()
    rows_two.finish_out()

    def sent_comb(k, _):
        comb_copy(k).wait_send()
        return 0

    lax.fori_loop(1, members, sent_comb, 0)
    for tile in weights:
        tile.sent()
    for i, (src, dst) in enumerate(stores):
        pltpu.make_async_copy(src, dst, store_sem.at[i]).wait()


def forward_call(
    grps, exps, lengths, bias_table, routes_t, tokens, cotangent, gains, router, attn_qkv, attn_out, expert_in, expert_out
):
    reps = grps * QUAD
    rows, width = tokens.shape
    head_cols = width // exps
    row_block, shard_cols = attn_qkv.shape
    seg = math.gcd(shard_cols, head_cols)
    segs = shard_cols // seg
    units = expert_out.shape[0]
    out_cols = attn_out.shape[1]
    heads = HEADS // exps
    members = QUAD * exps
    tiles = Tiles(units, reps)
    shape = jax.ShapeDtypeStruct
    vmem = pl.BlockSpec(memory_space=pltpu.VMEM)
    smem = pl.BlockSpec(memory_space=pltpu.SMEM)
    hbm = pl.BlockSpec(memory_space=pl.ANY)
    results = [
        (shape((2, width, 2 * tiles.size), low), hbm),
        (shape((2, tiles.size, width), low), hbm),
        (shape((members, rows, width), low), hbm),
        (shape((members, rows, width), low), hbm),
        (shape((members, 8, rows), full), hbm),
        (shape((exps, rows, 3 * head_cols), low), hbm),
        (shape((exps, rows, 128), full), hbm),
        (shape((exps, rows, head_cols), low), hbm),
        (shape((exps, rows, width), low), hbm),
        (shape((exps, 3 * head_cols, row_block), low), hbm),
        (shape((exps, reps, row_block, out_cols), low), hbm),
        (shape((rows, width), full), vmem),
        (shape((rows, width), low), vmem),
        (shape((rows, 128), full), vmem),
        (shape(expert_in.shape, low), hbm),
        (shape(expert_out.shape, low), hbm),
    ]
    dma = pltpu.SemaphoreType.DMA
    chips = members // 2
    return pl.pallas_call(
        functools.partial(forward_kernel, grps, exps),
        out_shape=[r[0] for r in results],
        in_specs=[smem] * 2 + [vmem] * 7 + [hbm] * 2,
        out_specs=[r[1] for r in results],
        scratch_shapes=[
            pltpu.VMEM(expert_in.shape, full),
            pltpu.VMEM(expert_out.shape, full),
            pltpu.VMEM((shard_cols, row_block), low),
            pltpu.VMEM((row_block, out_cols), low),
            pltpu.VMEM(expert_in.shape, low),
            pltpu.VMEM(expert_out.shape, low),
            pltpu.VMEM((exps, rows, width), low),
            pltpu.VMEM((exps, 3 * head_cols, row_block), low),
            pltpu.VMEM((exps, reps, row_block, out_cols), low),
            pltpu.VMEM((exps, rows, width), low),
            pltpu.VMEM((exps, rows, 3 * head_cols), low),
            pltpu.VMEM((exps, rows, 128), full),
            pltpu.VMEM((exps, rows, head_cols), low),
            pltpu.VMEM((exps, rows, head_cols), low),
            pltpu.VMEM((heads, rows, rows), full),
            pltpu.VMEM((8, rows), full),
            pltpu.VMEM((tiles.skip, width), low),
            dma((2, exps)),
            dma((2, max(segs * reps, exps * 3 * head_cols // seg))),
            dma((2, reps)),
            dma((2, exps)),
            dma((2, 2, 2 * reps)),
            dma((2, 2, reps + 1)),
            dma((2, exps)),
            dma((2, 3 * chips)),
            dma((2, 3 * chips + 1)),
            dma((2, 3 * chips)),
            dma((2, 3 * chips + 1)),
            dma((2, members)),
            dma((8,)),
            dma((2,)),
        ],
        compiler_params=pltpu.CompilerParams(
            collective_id=0, has_side_effects=True, vmem_limit_bytes=60 * 1024 * 1024
        ),
        name="forward",
    )(lengths, bias_table, routes_t, tokens, cotangent, gains, router, attn_qkv, attn_out, expert_in, expert_out)


def expert_kernel(
    grps,
    exps,
    cap,
    deal,
    routes_t,
    comb,
    n_all,
    cot_all,
    both_w,
    down_w,
    in_low,
    down_slab,
    h1,
    n_total,
    y_half,
    y_far,
    c_in,
    both_g,
    down_g,
    in_parts,
    down_parts,
    place,
    marks,
    n_rows,
    g_rows,
    both_v,
    down_v,
    raw_n,
    raw_g,
    y_acc,
    n_acc,
    both_d,
    active,
    n_bufs,
    c_sum,
    out_y,
    load_sem,
    raw_sem,
    out_sem,
    in_sem,
    in_down_sem,
    home_sem,
    home_down_sem,
    stage_sem,
    far_sem,
    n_sem,
    c_sem,
):
    at = Where(grps, exps)
    rows, width = n_all.shape[1:]
    tiles = Tiles(down_slab.shape[0], at.reps)
    size = tiles.size
    slots = exps * cap
    members = QUAD * exps
    loads = [pltpu.make_async_copy(both_w.at[t], both_v.at[t], load_sem.at[0, t]) for t in range(2)] + [
        pltpu.make_async_copy(down_w.at[t], down_v.at[t], load_sem.at[1, t]) for t in range(2)
    ]
    for copy in loads:
        copy.start()

    def raw_copies(q):
        here = pl.ds(pl.multiple_of(q * exps, exps), exps)
        return [
            pltpu.make_async_copy(n_all.at[here], raw_n.at[pl.ds(q % 2 * exps, exps)], raw_sem.at[0, q % 2]),
            pltpu.make_async_copy(cot_all.at[here], raw_g.at[pl.ds(q % 2 * exps, exps)], raw_sem.at[1, q % 2]),
        ]

    for copy in raw_copies(0):
        copy.start()

    beside = at.exp + 1 - 2 * (at.exp % 2)
    greet(*neighbours(at))()
    last = tiles.count - 1
    incoming = Outward(
        at, tiles, last, in_low, down_slab, both_v.at[last], down_v.at[last], None, in_sem, in_down_sem
    )
    incoming.start()
    home = Homeward(
        at, tiles, 0, both_v.at[0], down_v.at[0], in_parts, down_parts, home_sem, home_down_sem, (0,)
    )

    earlier = jnp.where(row_of((rows, rows)) < lane_of((rows, rows)), 1.0, 0.0).astype(low)
    slot = row_of((cap, rows)).astype(full)

    def dispatch(q, _):
        @pl.when(q + 1 < QUAD)
        def _():
            for copy in raw_copies(q + 1):
                copy.start()

        for copy in raw_copies(q):
            copy.wait()
        lines = []
        for j in range(exps):
            seq = at.grp * members + q * exps + j
            pair = routes_t[:, pl.ds(pl.multiple_of(seq * rows, rows), rows)]
            lines.append(jnp.logical_or(pair[0:1] == at.exp, pair[1:2] == at.exp))
        lines = [jnp.where(line, 1.0, 0.0) for line in lines] + [jnp.zeros((8 - exps, rows), full)]
        hot_low = jnp.concatenate(lines, axis=0).astype(low)
        before = dot(hot_low, earlier)
        for j in range(exps):
            s = q * exps + j
            inside = jnp.logical_and(slot == before[j : j + 1, :], hot_low[j : j + 1, :].astype(full) > 0.5)
            here = jnp.where(inside, 1.0, 0.0)
            place[s] = here.astype(low)
            g = raw_g[q % 2 * exps]
            for b in range(1, exps):
                g = jnp.where(deal[at.grp * members + s] == at.grp * members + q * exps + b, raw_g[q % 2 * exps + b], g)
            where = pl.ds(pl.multiple_of(s * cap, cap), cap)
            n_rows[where] = dot(here.astype(low), raw_n[q % 2 * exps + j]).astype(low)
            g_rows[where] = dot(here.astype(low), g).astype(low)
            marks[where, 0:1] = jnp.sum(here * comb[s, pl.ds(at.exp, 1), :], axis=1, keepdims=True)
            marks[where, 1:2] = jnp.zeros((cap, 1), full)
        return 0

    lax.fori_loop(0, QUAD, dispatch, 0)
    for copy in loads:
        copy.wait()
    curve = math.sqrt(2.0 / math.pi)

    core = at.exp % 2

    plane = at.quad * exps + at.exp
    sibling = at.device(at.rep, beside)
    dn = Halving(at, n_bufs, n_sem, [[0, 1, 2], [1, 2, 0], [2, 0, 1]])

    def n_copy(j):
        return send(raw_n.at[j], n_bufs[0].at[j], far_sem.at[0, 0, j], far_sem.at[0, 1, j], sibling)

    def y_copies(j):
        return (
            pltpu.make_async_copy(out_y.at[j % 2], y_half.at[j], out_sem.at[j % 2]),
            send(raw_n.at[j], y_far.at[j], far_sem.at[1, 0, j], far_sem.at[1, 1, j], sibling),
        )

    def c_copy(k):
        other = (plane + k) % members
        return send(
            c_sum.at[other],
            c_in.at[plane],
            c_sem.at[0, other],
            c_sem.at[1, plane],
            (at.grp, other // exps, other % exps),
        )

    def slots_of(s):
        return pl.ds(pl.multiple_of(s * cap, cap), cap)

    def n_rows_of(s):
        where = slots_of(s)
        line = jnp.sum(place[s].astype(full) * marks[where, 1:2], axis=0, keepdims=True)
        c_sum[s] = jnp.broadcast_to(line, (8, rows))
        return tn(place[s], n_acc[where]).astype(low)

    def y_rows_of(p):
        first = p // exps * exps
        spot = at.grp * members + p
        here, y = place[first], y_acc[slots_of(first)]
        for c in range(1, exps):
            taken = deal[at.grp * members + first + c] == spot
            here = jnp.where(taken, place[first + c], here)
            y = jnp.where(taken, y_acc[slots_of(first + c)], y)
        return (tn(here, y) + jnp.where(deal[at.me] == spot, h1[...], 0.0)).astype(low)

    def give_n(j, _):
        raw_n[j] = n_rows_of(2 * j + 1 - core)
        n_copy(j).start()
        raw_g[j] = n_rows_of(2 * j + core)
        return 0

    def add_n(j, _):
        arrived(n_bufs[0].at[j], far_sem.at[0, 1, j])
        n_bufs[0][j] = n_bufs[0][j] + raw_g[j]
        return 0

    def give_y(j, _):
        @pl.when(j >= 2)
        def _():
            y_copies(j - 2)[0].wait()

        out_y[j % 2] = y_rows_of(2 * j + core)
        n_copy(j).wait_send()
        raw_n[j] = y_rows_of(2 * j + 1 - core)
        for copy in y_copies(j):
            copy.start()
        return 0

    def start_c(k, _):
        c_copy(k).start()
        return 0

    def tile_work(f, _):
        @pl.when(f == last)
        def _():
            incoming.arrive()

        def chunk(c, _):
            here = pl.ds(pl.multiple_of(c * slots, slots), slots)
            share = marks[here, 0:1]
            both = dot(n_rows[here], both_v[f])
            gate_part, up_part = both[:, :size], both[:, size:]
            grad = nt(g_rows[here], down_v[f])
            square = gate_part * gate_part
            bend = jnp.tanh(curve * gate_part * (1.0 + 0.044715 * square))
            half = 0.5 * (1.0 + bend)
            gelu = gate_part * half
            slope = half + (0.5 * curve) * gate_part * (1.0 - bend * bend) * (1.0 + (3 * 0.044715) * square)
            value = gelu * up_part
            marks[here, 1:2] += jnp.sum(value * grad, axis=1, keepdims=True)
            grad = grad * share
            active[f, here] = (value * share).astype(low)
            both_d[f, here, :size] = (grad * up_part * slope).astype(low)
            both_d[f, here, size:] = (grad * gelu).astype(low)
            y = dot(active[f, here], down_v[f])
            y_acc[here] = jnp.where(f == 0, y, y_acc[here].astype(full) + y).astype(low)
            n_back = nt(both_d[f, here], both_v[f])
            n_acc[here] = jnp.where(f == 0, n_back, n_acc[here].astype(full) + n_back).astype(low)
            return 0

        lax.fori_loop(0, QUAD, chunk, 0)

        return 0

    def weight_work(f):
        def columns(m, _):
            cols = pl.ds(pl.multiple_of(m * (width // 2), width // 2), width // 2)
            both_v[f, cols] = tn(n_rows[:, cols], both_d[f]).astype(low)
            down_v[f, :, cols] = tn(active[f], g_rows[:, cols]).astype(low)
            return 0

        lax.fori_loop(0, 2, columns, 0)

        for copy in stage_copies(f):
            copy.start()
        if f == 0:
            home.start()

    def stage_copies(f):
        copies = [pltpu.make_async_copy(both_v.at[f], both_g.at[f], stage_sem.at[0, f])]
        if f:
            copies.append(pltpu.make_async_copy(down_v.at[f], down_g.at[f - 1], stage_sem.at[1, f]))
        return copies

    lax.fori_loop(0, tiles.count, tile_work, 0)

    half = members // 2
    lax.fori_loop(0, half, give_n, 0)
    lax.fori_loop(1, members, start_c, 0)
    c_in[plane] = c_sum[plane]
    weight_work(0)
    lax.fori_loop(0, half, add_n, 0)
    dn.start(0)
    weight_work(1)
    dn.next(0)
    weight_work(2)
    dn.next(1)
    lax.fori_loop(0, half, give_y, 0)
    for step in range(2, len(dn.chip_bits)):
        dn.next(step)
    n_total[...] = dn.result()[0]
    for j in (half - 2, half - 1):
        y_copies(j)[0].wait()
    for f in range(tiles.count):
        for copy in stage_copies(f):
            copy.wait()

    def core_in(j, _):
        y_copies(j)[1].wait_send()
        arrived(y_far.at[j], far_sem.at[1, 1, j])
        return 0

    lax.fori_loop(0, half, core_in, 0)

    def c_done(k, _):
        c_copy(k).wait_send()
        other = (plane + k) % members
        arrived(c_in.at[other], c_sem.at[1, other])
        return 0

    lax.fori_loop(1, members, c_done, 0)
    dn.finish()
    home.arrive()
    incoming.sent()
    home.sent()


def expert_call(grps, exps, cap, deal, routes_t, comb_all, n_all, cot_all, both_w, down_w, in_low, down_slab, h1):
    members, rows, width = n_all.shape
    reps = grps * QUAD
    tiles = Tiles(down_slab.shape[0], reps)
    size = tiles.size
    slab, both_hidden = in_low.shape
    units = down_slab.shape[0]
    slots = exps * cap
    chip_bits = bits_of(members) - 1
    shape = jax.ShapeDtypeStruct
    vmem = pl.BlockSpec(memory_space=pltpu.VMEM)
    smem = pl.BlockSpec(memory_space=pltpu.SMEM)
    hbm = pl.BlockSpec(memory_space=pl.ANY)
    results = [
        (shape((rows, width), low), vmem),
        (shape((members // 2, rows, width), low), hbm),
        (shape((members // 2, rows, width), low), hbm),
        (shape((members, 8, rows), full), vmem),
        (shape((tiles.count, width, 2 * size), low), hbm),
        (shape((2, size, width), low), hbm),
        (shape((grps, slab, both_hidden), low), hbm),
        (shape((grps, units, width), low), hbm),
    ]
    dma = pltpu.SemaphoreType.DMA
    return pl.pallas_call(
        functools.partial(expert_kernel, grps, exps, cap),
        out_shape=[r[0] for r in results],
        in_specs=[smem] + [vmem] * 2 + [hbm] * 6 + [vmem],
        out_specs=[r[1] for r in results],
        scratch_shapes=[
            pltpu.VMEM((members, cap, rows), low),
            pltpu.VMEM((QUAD * slots, 128), full),
            pltpu.VMEM((QUAD * slots, width), low),
            pltpu.VMEM((QUAD * slots, width), low),
            pltpu.VMEM((tiles.count, width, 2 * size), low),
            pltpu.VMEM((tiles.count, size, width), low),
            pltpu.VMEM((2 * exps, rows, width), low),
            pltpu.VMEM((2 * exps, rows, width), low),
            pltpu.VMEM((QUAD * slots, width), low),
            pltpu.VMEM((QUAD * slots, width), low),
            pltpu.VMEM((tiles.count, QUAD * slots, 2 * size), low),
            pltpu.VMEM((tiles.count, QUAD * slots, size), low),
            [pltpu.VMEM((members >> (1 + step), rows, width), low) for step in range(chip_bits + 1)],
            pltpu.VMEM((members, 8, rows), full),
            pltpu.VMEM((2, rows, width), low),
            dma((2, 2)),
            dma((2, 2)),
            dma((2,)),
            dma((2, 2 * reps)),
            dma((2, reps + 1)),
            dma((2, 2 * reps)),
            dma((2, max(QUAD, grps))),
            dma((2, tiles.count)),
            dma((2, 2, members // 2)),
            dma((2, 3 << chip_bits)),
            dma((2, members)),
        ],
        compiler_params=pltpu.CompilerParams(
            collective_id=2, has_side_effects=True, vmem_limit_bytes=60 * 1024 * 1024
        ),
        name="experts",
    )(deal, routes_t, comb_all, n_all, cot_all, both_w, down_w, in_low, down_slab, h1)


def adamw_root(weight, moment, second, gradient, step_rate, decay_factor):
    new_moment = beta_one * moment + (1.0 - beta_one) * gradient
    new_second = beta_two * second + (1.0 - beta_two) * gradient * gradient
    root = lax.rsqrt(new_second * (1.0 / (1.0 - beta_two**STEP)))
    step = new_moment * (root * (1.0 - eps_adam * root))
    keep = 1.0 - step_rate * decay_factor
    return (new_moment, new_second, keep * weight - (step_rate / (1.0 - beta_one**STEP)) * step)


def adam_kernel(exps, *refs):
    in_parts, down_parts, qkv_grad, out_grad, small = refs[:5]
    states, news, bias_grad = refs[5:26], refs[26:47], refs[47]
    heads = HEADS // exps
    width = small.shape[1]

    def update(i, grad, rate, decay):
        weight, first, second = [state[...] for state in states[3 * i : 3 * i + 3]]
        values = adamw_root(weight, first, second, grad, rate, decay)
        for new, value in zip(news[3 * i : 3 * i + 3], values, strict=True):
            new[...] = value

    def total(parts):
        result = parts[0].astype(full)
        for k in range(1, parts.shape[0]):
            result = result + parts[k].astype(full)
        return result

    @pl.when(pl.program_id(0) == 0)
    def _():
        update(0, qkv_grad[...], 1.5 / math.sqrt(D), 0.1)
        update(1, out_grad[...], 6.0 / math.sqrt(D), 0.1)
        for e in range(exps):
            for h in range(heads):
                bias_grad[e * heads + h : e * heads + h + 1, :] = small[
                    exps + 3 + e : exps + 4 + e, h * 128 : h * 128 + BUCKETS
                ]
        update(2, bias_grad[...], 0.3, 0.0)
        update(3, small[0:exps, :], 1.0 / math.sqrt(D), 0.1)
        update(4, small[exps : exps + 2, :], 0.5, 0.0)

    update(5, total(in_parts), 1.5 / math.sqrt(D), 0.1)
    update(6, total(down_parts), 1.5 / math.sqrt(FF), 0.1)


def adam_call(exps, in_parts, down_parts, qkv_grad, out_grad, small, states):
    steps = 4

    def whole(array):
        return pl.BlockSpec(array.shape, lambda i: (0,) * array.ndim)

    def columns(array):
        block = array.shape[:-1] + (array.shape[-1] // steps,)
        return pl.BlockSpec(block, lambda i: (0,) * (array.ndim - 1) + (i,))

    specs = [whole(state) for state in states[:15]]
    specs += [columns(state) for state in states[15:18]] + [columns(state) for state in states[18:]]
    return pl.pallas_call(
        functools.partial(adam_kernel, exps),
        grid=(steps,),
        in_specs=[columns(in_parts), columns(down_parts), whole(qkv_grad), whole(out_grad), whole(small)] + specs,
        out_specs=specs,
        out_shape=[jax.ShapeDtypeStruct(state.shape, full) for state in states],
        scratch_shapes=[pltpu.VMEM((HEADS, BUCKETS), full)],
        compiler_params=pltpu.CompilerParams(vmem_limit_bytes=60 * 1024 * 1024),
        name="adam",
    )(in_parts, down_parts, qkv_grad, out_grad, small, *states)


def backward_kernel(
    grps,
    exps,
    lengths,
    deal,
    bias_table,
    y_half,
    y_far,
    both_g,
    down_g,
    in_before,
    down_before,
    n1_in,
    cot_all,
    routes_t,
    tokens,
    n_total,
    c_in,
    n2_in,
    probs_in,
    h1_from,
    qkv_from,
    lse_from,
    mine_from,
    wqkv_from,
    wout_from,
    gains,
    router_t,
    *rest,
):
    token_grad, block_out, in_parts, down_parts, qkv_grad, out_grad, small_out = rest[:7]
    scratch = rest[7:]
    (
    h1_in,
    qkv,
    lse,
    mine,
    wqkv,
    wout,
    kept,
    y_bufs,
    dh1,
    dz_send,
    dz_all,
    do_send,
    do_in,
    bias,
    bias_sum,
    dqkv,
    dqkv_t,
    dn1_send,
    dn1_in,
    wq_send,
    og_send,
    mids,
    far_send,
    far_in,
    small_send,
    small_exp,
    small_sum,
    small_rep,
    y_sem,
    load_sem,
    weight_sem,
    down_sem,
    dz_sem,
    do_sem,
    dn1_sem,
    wq_sem,
    og_sem,
    mid_sem,
    far_sem,
    small_sem,
    small2_sem,
    n1_sem,
    operand_sem,
    ) = scratch
    at = Where(grps, exps)
    reps = at.reps
    rows, width = tokens.shape
    heads = HEADS // exps
    head_dim = width // HEADS
    head_cols = heads * head_dim
    block_cols = min(128, head_cols)
    row_block = wqkv.shape[2]
    out_cols = wout.shape[3]
    tiles = Tiles(down_parts.shape[1], reps)
    scale = 1.0 / math.sqrt(head_dim)
    SEND, RECV = 0, 1
    plane = at.quad * exps + at.exp
    members = QUAD * exps

    def exp_peer(k):
        return (at.exp + k) % exps

    router = router_t[...]
    met = greet(*neighbours(at))
    n1 = kept.at[0:exps]
    group = pl.ds(pl.multiple_of(at.quad * exps, exps), exps)
    cot_copy = pltpu.make_async_copy(cot_all.at[group], dn1_send, n1_sem.at[1])
    cot_copy.start()
    loads = [
        pltpu.make_async_copy(src, dst, operand_sem.at[i])
        for i, (src, dst) in enumerate(
            ((h1_from, h1_in), (wout_from, wout), (qkv_from, qkv), (lse_from, lse), (mine_from, mine), (wqkv_from, wqkv))
        )
    ]
    ys = Halving(at, y_bufs, y_sem, [[0, 1, 2], [0, 1, 2], [1, 0, 2]])
    half_loads = [
        pltpu.make_async_copy(y_far, y_bufs[0], load_sem.at[0]),
        pltpu.make_async_copy(y_half, kept, load_sem.at[1]),
    ]
    for copy in loads + half_loads:
        copy.start()

    span = 2 * rows
    bucket = bucket_of(lane_of((8, span)) - rows)
    for h in range(heads):
        line = jnp.zeros((8, span), full)
        for b in range(BUCKETS):
            line = jnp.where(bucket == b, bias_table[at.exp * heads + h, b], line)
        whole = jnp.broadcast_to(line[0:1], (rows, span))
        bias[h] = pltpu.roll(whole, 0, 1, stride=1, stride_axis=0)[:, rows:]


    met()

    homes = [
        Homeward(
            at,
            tiles,
            t,
            both_g.at[t],
            down_g.at[t - 1] if t else None,
            in_parts,
            down_parts,
            weight_sem.at[t],
            down_sem.at[t],
            (0, 1) if t else (1,),
        )
        for t in range(tiles.count)
    ]
    homes[0].start()
    homes[1].start()
    n1_copy = pltpu.make_async_copy(n1_in, n1, n1_sem.at[0])

    lane = lane_of((rows, 128))
    comb_rows = []
    for e in range(exps):
        total = c_in[e]
        for q in range(1, QUAD):
            total = total + c_in[q * exps + e]
        comb_rows.append(total[0:1, :])
    comb_rows.append(jnp.zeros((128 - exps, rows), full))
    comb_grad = jnp.concatenate(comb_rows, axis=0).T
    valid = row_of((rows, 1)) < lengths[at.me]
    probs = probs_in[...]
    hot = routed(routes_t, at.me, rows)
    picked = jnp.where(hot, probs, 0.0)
    total = jnp.sum(picked, axis=1, keepdims=True)
    gate = picked / total
    gate_grad_rows = jnp.where(valid, comb_grad, 0.0)
    spread_grad = jnp.sum(gate_grad_rows * gate, axis=1, keepdims=True)
    probs_grad = jnp.where(hot, (gate_grad_rows - spread_grad) / total, 0.0)
    logit_grad = probs * (probs_grad - jnp.sum(probs_grad * probs, axis=1, keepdims=True))
    small_rows = small_send.shape[0]
    small_send[...] = jnp.zeros_like(small_send)
    router_back = jnp.dot(
        logit_grad, jnp.concatenate([router, jnp.zeros((128 - exps, width), full)], axis=0),
        precision=highest, preferred_element_type=full,
    )
    for copy in loads:
        copy.wait()
    h1 = h1_in[...]
    r2 = lax.rsqrt(jnp.mean(h1 * h1, axis=1, keepdims=True) + eps_norm)

    steps = len(ys.chip_bits)
    n2_grad = router_back + n_total[...].astype(full)
    scaled = n2_grad * gains[1:2, :]
    cot_copy.wait()
    dealt = deal[at.me] - at.base
    g = dn1_send[0]
    for e in range(1, exps):
        g = jnp.where(dealt == e, dn1_send[e], g)
    hidden_grad = (
        jnp.where(valid, g.astype(full), 0.0)
        + r2 * scaled
        - h1 * (r2 * r2 * r2) * jnp.mean(scaled * h1, axis=1, keepdims=True)
    )
    dh1[...] = hidden_grad
    small_send[exps + 1 : exps + 2, :] = jnp.sum(n2_grad * h1 * r2, axis=0, keepdims=True)
    branch = hidden_grad.astype(low)
    dz_send[...] = branch
    for e in range(exps):
        total = jnp.zeros((rows, row_block), full)
        for r in range(reps):
            total = total + nt(branch[:, r * out_cols : (r + 1) * out_cols], wout[e, r])
        do_send[e] = total.astype(low)

    def do_copies():
        return [
            send(
                do_send.at[exp_peer(k)],
                do_in.at[at.exp],
                do_sem.at[SEND, exp_peer(k)],
                do_sem.at[RECV, at.exp],
                at.device(at.rep, exp_peer(k)),
            )
            for k in range(1, exps)
        ]

    for copy in do_copies():
        copy.start()
    pltpu.make_async_copy(do_send.at[at.exp], do_in.at[at.exp], do_sem.at[RECV, at.exp]).start()

    group_dz = Group(at, dz_send, dz_all, dz_sem)
    group_dz.start()
    dz_all[at.exp] = branch
    for copy in half_loads:
        copy.wait()

    def add_halves(j, _):
        y_bufs[0][j] = y_bufs[0][j] + kept[j]
        return 0

    lax.fori_loop(0, kept.shape[0], add_halves, 0)
    ys.start(0)
    n1_copy.start()

    bias_sum[...] = jnp.zeros_like(bias_sum)

    def dn1_copies():
        beside, across = turn(at.exp, 2), turn(at.exp, 1)
        return [
            functools.partial(
                send, dn1_send.at[k], dn1_in.at[j], dn1_sem.at[SEND, j], dn1_sem.at[RECV, j], at.device(at.rep, to)
            )
            for k, j, to in ((turn(at.exp, 0), 2, beside), (across, 0, across), (beside, 1, beside))
        ]

    def attend_back(i, _):
        s = turn(at.exp, i)
        @pl.when(i == 1)
        def _():
            group_dz.pass_on()

        arrived(do_in.at[s], do_sem.at[RECV, s])
        ok = lane_of((rows, rows)) < lengths[at.base + s]
        block_lane = lane_of((rows, block_cols))
        for c in range(head_cols // block_cols):
            cols = slice(c * block_cols, (c + 1) * block_cols)
            k_cols = slice(head_cols + c * block_cols, head_cols + (c + 1) * block_cols)
            v_cols = slice(2 * head_cols + c * block_cols, 2 * head_cols + (c + 1) * block_cols)
            q = qkv[s, :, cols] * scale
            k = qkv[s, :, k_cols]
            v = qkv[s, :, v_cols]
            do = do_in[s, :, cols]
            dq = jnp.zeros((rows, block_cols), full)
            dk = jnp.zeros((rows, block_cols), full)
            dv = jnp.zeros((rows, block_cols), full)
            for t in range(block_cols // head_dim):
                h = c * (block_cols // head_dim) + t
                here = jnp.logical_and(block_lane >= t * head_dim, block_lane < (t + 1) * head_dim)
                zero = jnp.zeros_like(q)
                q_h = jnp.where(here, q, zero)
                do_h = jnp.where(here, do, zero)
                scores = nt(q_h, k) + bias[h]
                p = jnp.where(ok, jnp.exp(scores - lse[s, :, h : h + 1]), 0.0)
                dp = nt(do_h, v)
                delta = jnp.sum(dp * p, axis=1, keepdims=True)
                ds = (p * (dp - delta)).astype(low)
                bias_sum[h] += ds.astype(full)
                dv = jnp.where(here, tn(p.astype(low), do), dv)
                dq = jnp.where(here, jnp.dot(ds, k, preferred_element_type=full), dq)
                dk = jnp.where(here, tn(ds, q), dk)
            dqkv[:, cols] = (dq * scale).astype(low)
            dqkv[:, k_cols] = dk.astype(low)
            dqkv[:, v_cols] = dv.astype(low)
        dqkv_t[:, pl.ds(pl.multiple_of(s * rows, rows), rows)] = dqkv[...].T
        for e in range(exps):
            dn1_send[s, :, e * row_block : (e + 1) * row_block] = jnp.dot(
                dqkv[...], wqkv[e], preferred_element_type=full
            ).astype(low)

        @pl.when(i == 0)
        def _():
            dn1_copies()[0]().start()

        @pl.when(i == 1)
        def _():
            arrived(dn1_in.at[2], dn1_sem.at[RECV, 2])
            dn1_send[s] = (dn1_send[s].astype(full) + dn1_in[2].astype(full)).astype(low)
            dn1_copies()[1]().start()

        @pl.when(i == 2)
        def _():
            dn1_copies()[2]().start()

        return 0

    lax.fori_loop(0, exps, attend_back, 0)

    n1_copy.wait()
    seg = wq_send.shape[2]
    parts = wq_send.shape[1]
    segs = mids.shape[1] - 1
    for e in range(exps):
        part = kept[0:exps, :, e * row_block : (e + 1) * row_block].reshape(exps * rows, row_block)
        total = dot(dqkv_t[...], part)
        for j in range(parts):
            wq_send[e, j] = total[j * seg : (j + 1) * seg].astype(low)

    def owner(j):
        section, within = j // (head_cols // seg), j % (head_cols // seg)
        col = section * width + at.exp * head_cols + within * seg
        block = col // seg
        return block // segs, block % segs

    def mid_place(grp, k, quad):
        return (grp * (segs + 1) + k) * QUAD + quad

    def mid_copy(src, send_sem, rep, k, e):
        dst = mids.at[rep // QUAD, k, at.quad]
        recv = mid_sem.at[mid_place(rep // QUAD, k, at.quad)]
        stays = jnp.logical_and(rep % QUAD == at.quad, e == at.exp)
        return (
            stays,
            functools.partial(send, src, dst, send_sem, recv, (at.grp, rep % QUAD, e)),
            functools.partial(pltpu.make_async_copy, src, dst, recv),
        )

    def wq_copy(i):
        e, j = i // parts, i % parts
        rep, k = owner(j)
        return mid_copy(wq_send.at[e, j], wq_sem.at[i], rep, k, e)

    def og_copy(r):
        return mid_copy(og_send.at[r], og_sem.at[r], r, segs, at.exp)

    def go(copies, act, act_local):
        stays, away, local = copies

        @pl.when(jnp.logical_not(stays))
        def _():
            act(away)

        if act_local:

            @pl.when(stays)
            def _():
                act_local(local)

    def over(count, copies, act, act_local):
        def one(i, _):
            go(copies(i), act, act_local)
            return 0

        lax.fori_loop(0, count, one, 0)

    over(exps * parts, wq_copy, lambda copy: copy().start(), lambda copy: copy().start())
    group_dz.arrive()
    grad = tn(mine[...].reshape(exps * rows, head_cols), dz_all[...].reshape(exps * rows, width))
    for r in range(reps):
        og_send[r] = grad[:, r * out_cols : (r + 1) * out_cols].T.astype(low)
    over(reps, og_copy, lambda copy: copy().start(), lambda copy: copy().start())
    homes[2].start()

    n1_grad = dn1_send[at.exp].astype(full)
    for j in range(2):
        arrived(dn1_in.at[j], dn1_sem.at[RECV, j])
        n1_grad = n1_grad + dn1_in[j].astype(full)
    x = tokens[...].astype(full)
    r1 = lax.rsqrt(jnp.mean(x * x, axis=1, keepdims=True) + eps_norm)
    scaled = n1_grad * gains[0:1, :]
    token_grad[...] = (
        dh1[...] + r1 * scaled - x * (r1 * r1 * r1) * jnp.mean(scaled * x, axis=1, keepdims=True)
    )
    small_send[exps : exps + 1, :] = jnp.sum(n1_grad * x * r1, axis=0, keepdims=True)

    router_rows = lax.dot_general(
        logit_grad, n2_in[...].astype(full), (((0,), (0,)), ((), ())), preferred_element_type=full, precision=highest
    )
    small_send[0:exps, :] = router_rows[0:exps, :]

    line_lane = lane_of((8, 128))
    line_row = row_of((8, 128))
    bias_line = jnp.zeros((8, 128), full)
    flip = jnp.where(row_of((rows, rows)) + lane_of((rows, rows)) == rows - 1, 1.0, 0.0).astype(low)
    turned_bucket = bucket_of(rows - 1 - lane_of((8, span)))
    for h in range(heads):
        high = bias_sum[h].astype(low)
        rest = (bias_sum[h] - high.astype(full)).astype(low)
        flipped = dot(high, flip) + dot(rest, flip)
        square = jnp.concatenate([flipped, jnp.zeros((rows, rows), full)], axis=1)
        turned = pltpu.roll(square, 0, 1, stride=1, stride_axis=0)
        sums = jnp.broadcast_to(jnp.sum(turned, axis=0, keepdims=True), (8, span))
        for b in range(BUCKETS):
            value = jnp.sum(jnp.where(turned_bucket == b, sums, 0.0), axis=1, keepdims=True)
            bias_line = jnp.where(jnp.logical_and(line_row == h, line_lane == b), value, bias_line)
    for h in range(heads):
        small_send[exps + 2 : exps + 3, h * 128 : (h + 1) * 128] = bias_line[h : h + 1, :]

    def small_copies():
        return [
            send(
                small_send,
                small_exp.at[at.exp],
                small_sem.at[SEND, exp_peer(k)],
                small_sem.at[RECV, at.exp],
                at.device(at.rep, exp_peer(k)),
            )
            for k in range(1, exps)
        ]

    for copy in small_copies():
        copy.start()
    small_exp[at.exp] = small_send[...]
    ys.next(0)

    def mid_sum(grp, k):
        for q in range(QUAD):
            arrived(mids.at[grp, k, q], mid_sem.at[mid_place(grp, k, q)])
        total = mids[grp, k, 0].astype(full)
        for q in range(1, QUAD):
            total = total + mids[grp, k, q].astype(full)
        return total

    far = 1 - at.grp
    for k in range(segs + 1):
        far_send[k] = mid_sum(far, k).astype(low)

    def far_copy():
        return send(far_send, far_in, far_sem.at[SEND], far_sem.at[RECV], (far, at.quad, at.exp))

    far_copy().start()
    ys.next(1)
    for k in range(1, exps):
        arrived(small_exp.at[exp_peer(k)], small_sem.at[RECV, exp_peer(k)])
    total = small_exp[0]
    for e in range(1, exps):
        total = total + small_exp[e]
    small_sum[0] = total
    for e in range(exps):
        small_sum[0, exps + 3 + e : exps + 4 + e, :] = small_exp[e, exps + 2 : exps + 3, :]

    def small2_copies():
        return [
            send(
                small_sum.at[0],
                small_rep.at[at.rep],
                small2_sem.at[SEND, (at.rep + k) % reps],
                small2_sem.at[RECV, at.rep],
                at.device((at.rep + k) % reps, at.exp),
            )
            for k in range(1, reps)
        ]

    for copy in small2_copies():
        copy.start()
    small_rep[at.rep] = small_sum[0]
    for step in range(2, steps):
        ys.next(step)
    length = lengths[at.base]
    for e in range(1, exps):
        length = jnp.where(deal[at.base + e] == at.me, lengths[at.base + e], length)
    block = ys.result()[0]
    block_out[...] = jnp.where(row_of((rows, 1)) < length, block, jnp.zeros_like(block))
    for k in range(1, reps):
        arrived(small_rep.at[(at.rep + k) % reps], small2_sem.at[RECV, (at.rep + k) % reps])
    total = small_rep[0]
    for r in range(1, reps):
        total = total + small_rep[r]
    small_out[...] = total

    near = [mid_sum(at.grp, k) for k in range(segs + 1)]
    arrived(far_in, far_sem.at[RECV])
    grads = [(near[k] + far_in[k].astype(full)).T for k in range(segs + 1)]
    qkv_grad[...] = jnp.concatenate(grads[:segs], axis=1)
    out_grad[...] = grads[segs]
    for home in homes:
        home.arrive()

    ys.finish()

    for home in homes:
        home.sent()

    over(exps * parts, wq_copy, lambda copy: copy().wait_send(), None)
    over(reps, og_copy, lambda copy: copy().wait_send(), None)
    far_copy().wait_send()
    for copies in (do_copies(), small_copies(), small2_copies()):
        for copy in copies:
            copy.wait_send()
    for copy in dn1_copies():
        copy().wait_send()
    group_dz.sent()


def routed(routes_t, seq, rows):
    pair = routes_t[:, pl.ds(pl.multiple_of(seq * rows, rows), rows)].astype(full)
    cols = jnp.concatenate([pair, jnp.zeros((126, rows), full)], axis=0).T
    lane = lane_of((rows, 128)).astype(full)
    return jnp.logical_or(lane == cols[:, 0:1], lane == cols[:, 1:2])


def backward_call(
    grps, exps, lengths, deal, bias_table, y_half, y_far, both_g, down_g, in_before, down_before, n1,
    cot_all, routes_t, tokens, n_total, c_in, n2, probs, h1, qkv, lse, mine, wqkv, wout, gains, router
):
    reps = grps * QUAD
    rows, width = tokens.shape
    heads = HEADS // exps
    head_cols = width // exps
    row_block = wqkv.shape[2]
    out_cols = wout.shape[3]
    shard_cols = 3 * width // reps
    seg = math.gcd(shard_cols, head_cols)
    segs = shard_cols // seg
    parts = 3 * head_cols // seg
    members = QUAD * exps
    chip_bits = bits_of(members) - 1
    small_rows = -(-(2 * exps + 3) // 8) * 8
    shape = jax.ShapeDtypeStruct
    vmem = pl.BlockSpec(memory_space=pltpu.VMEM)
    smem = pl.BlockSpec(memory_space=pltpu.SMEM)
    hbm = pl.BlockSpec(memory_space=pl.ANY)
    results = [
        (shape((rows, width), full), vmem),
        (shape((rows, width), low), vmem),
        (shape(in_before.shape, low), hbm),
        (shape(down_before.shape, low), hbm),
        (shape((row_block, shard_cols), full), vmem),
        (shape((row_block, out_cols), full), vmem),
        (shape((small_rows, width), full), vmem),
    ]
    dma = pltpu.SemaphoreType.DMA
    bufs = [pltpu.VMEM((1 << (chip_bits - s), rows, width), low) for s in range(chip_bits + 1)]
    return pl.pallas_call(
        functools.partial(backward_kernel, grps, exps),
        out_shape=[r[0] for r in results],
        in_specs=[smem] * 3 + [hbm] * 8 + [vmem] * 6 + [hbm] * 6 + [vmem] * 2,
        out_specs=[r[1] for r in results],
        scratch_shapes=[
            pltpu.VMEM(h1.shape, full),
            pltpu.VMEM(qkv.shape, low),
            pltpu.VMEM(lse.shape, full),
            pltpu.VMEM(mine.shape, low),
            pltpu.VMEM(wqkv.shape, low),
            pltpu.VMEM(wout.shape, low),
            pltpu.VMEM((members // 2, rows, width), low),
            list(bufs),
            pltpu.VMEM((rows, width), full),
            pltpu.VMEM((rows, width), low),
            pltpu.VMEM((exps, rows, width), low),
            pltpu.VMEM((exps, rows, head_cols), low),
            pltpu.VMEM((exps, rows, head_cols), low),
            pltpu.VMEM((heads, rows, rows), full),
            pltpu.VMEM((heads, rows, rows), full),
            pltpu.VMEM((rows, 3 * head_cols), low),
            pltpu.VMEM((3 * head_cols, exps * rows), low),
            pltpu.VMEM((exps, rows, width), low),
            pltpu.VMEM((3, rows, width), low),
            pltpu.VMEM((exps, parts, seg, row_block), low),
            pltpu.VMEM((reps, seg, row_block), low),
            pltpu.VMEM((grps, segs + 1, QUAD, seg, row_block), low),
            pltpu.VMEM((segs + 1, seg, row_block), low),
            pltpu.VMEM((segs + 1, seg, row_block), low),
            pltpu.VMEM((small_rows, width), full),
            pltpu.VMEM((exps, small_rows, width), full),
            pltpu.VMEM((1, small_rows, width), full),
            pltpu.VMEM((reps, small_rows, width), full),
            dma((2, 3 << chip_bits)),
            dma((2,)),
            dma((3, 2, 2 * reps)),
            dma((3, 2, max(QUAD, grps))),
            dma((2, exps)),
            dma((2, exps)),
            dma((2, exps)),
            dma((exps * parts,)),
            dma((reps,)),
            dma((grps * (segs + 1) * QUAD,)),
            dma((2,)),
            dma((2, exps)),
            dma((2, reps)),
            dma((2,)),
            dma((6,)),
        ],
        compiler_params=pltpu.CompilerParams(
            collective_id=1, has_side_effects=True, vmem_limit_bytes=60 * 1024 * 1024
        ),
        input_output_aliases={7: 2, 8: 3},
        name="backward",
    )(
        lengths, deal, bias_table, y_half, y_far, both_g, down_g, in_before, down_before, n1, cot_all,
        routes_t, tokens, n_total, c_in, n2, probs, h1, qkv, lse, mine, wqkv, wout, gains, router
    )


def per_device(
    tokens,
    cotangent,
    seq_lengths,
    deal,
    routes,
    attn_qkv,
    qkv_first,
    qkv_second,
    attn_out,
    out_first,
    out_second,
    rel_bias,
    bias_first,
    bias_second,
    router,
    router_first,
    router_second,
    norm_gains,
    gains_first,
    gains_second,
    expert_in,
    in_first,
    in_second,
    expert_out,
    down_first,
    down_second,
):
    rows, width = tokens.shape
    experts = router.shape[1]
    capacity = (10 * rows + 4 * experts - 1) // (4 * experts)
    exps = lax.axis_size("exp")
    grps = lax.axis_size("grp")
    routes_t = routes.T
    bias_table = rel_bias.T
    (
        both_w, down_w, cot_all, n_all, comb_all, qkv, lse, context_mine, normed_group, wqkv, wout, hidden_one,
        normed_two, router_probs, in_low, down_low,
    ) = forward_call(
        grps, exps, seq_lengths, bias_table, routes_t, tokens, cotangent, norm_gains.T, router.T,
        attn_qkv, attn_out, expert_in[0], expert_out[0],
    )
    n_total, y_half, y_far, c_in, both_g, down_g, in_before, down_before = expert_call(
        grps, exps, capacity, deal, routes_t, comb_all, n_all, cot_all, both_w, down_w, in_low, down_low,
        hidden_one,
    )
    token_grad, block_out, in_parts, down_parts, qkv_grad, out_grad, small = backward_call(
        grps, exps, seq_lengths, deal, bias_table, y_half, y_far, both_g, down_g,
        in_before, down_before, normed_group, cot_all, routes_t, tokens, n_total, c_in, normed_two, router_probs, hidden_one, qkv, lse, context_mine, wqkv,
        wout, norm_gains.T, router.T,
    )
    states = [
        attn_qkv, qkv_first, qkv_second, attn_out, out_first, out_second, bias_table, bias_first.T, bias_second.T,
        router.T, router_first.T, router_second.T, norm_gains.T, gains_first.T, gains_second.T,
        expert_in[0], in_first[0], in_second[0], expert_out[0], down_first[0], down_second[0],
    ]
    new = list(adam_call(exps, in_parts, down_parts, qkv_grad, out_grad, small, states))
    new = new[:6] + [array.T for array in new[6:15]] + [array[None] for array in new[15:]]
    return (block_out, token_grad, *new)


def bucket_onehot(length):
    places = jnp.arange(length, dtype=jnp.int32)
    offset = places[None, :] - places[:, None]
    distance = jnp.abs(offset)
    bucket = 16 * (offset > 0).astype(jnp.int32)
    for threshold in thresholds:
        bucket = bucket + (distance >= threshold).astype(jnp.int32)
    return (bucket[:, :, None] == jnp.arange(BUCKETS, dtype=jnp.int32)[None, None, :]).astype(full)


def swap(pieces, axes):
    return lax.all_to_all(pieces, axes, split_axis=0, concat_axis=0, tiled=True)


def spread(block, axes):
    members = lax.axis_size(axes)
    return swap(jnp.broadcast_to(block[None], (members,) + block.shape), axes)


def plain_device(
    tokens,
    cotangent,
    seq_lengths,
    deal,
    routes,
    attn_qkv,
    qkv_first,
    qkv_second,
    attn_out,
    out_first,
    out_second,
    rel_bias,
    bias_first,
    bias_second,
    router,
    router_first,
    router_second,
    norm_gains,
    gains_first,
    gains_second,
    expert_in,
    in_first,
    in_second,
    expert_out,
    down_first,
    down_second,
):
    rows, width = tokens.shape
    head_dim = width // HEADS
    score_scale = 1.0 / math.sqrt(head_dim)
    experts = router.shape[1]
    capacity = (10 * rows + 4 * experts - 1) // (4 * experts)
    exps = lax.axis_size("exp")
    grps = lax.axis_size("grp")
    reps = grps * QUAD
    heads = HEADS // exps
    head_cols = heads * head_dim
    place = lax.axis_index("exp")
    base = lax.axis_index(REP) * exps
    me = base + place
    slab = expert_in.shape[1]
    units = expert_out.shape[1]
    quarter = grps * units

    row_block = attn_qkv.shape[0]
    qkv_rows = lax.all_gather(attn_qkv.astype(low), REP, axis=1, tiled=True)
    out_rows = lax.all_gather(attn_out.astype(low), REP, axis=1, tiled=True)
    qkv_pieces = jnp.transpose(
        qkv_rows.reshape(row_block, 3, exps, head_cols), (2, 0, 1, 3)
    ).reshape(exps, row_block, 3 * head_cols)
    qkv_mine = swap(qkv_pieces, "exp").reshape(width, 3 * head_cols)
    full_out = spread(out_rows, "exp").reshape(width, width)

    group_tokens = spread(tokens, "exp")
    group_cotangent = spread(cotangent, "exp")
    my_cotangent = lax.dynamic_index_in_dim(group_cotangent, deal[me] - base, 0, keepdims=False)

    my_routes = lax.dynamic_slice_in_dim(routes, me * rows, rows, 0)
    places = jnp.arange(rows, dtype=jnp.int32)
    valid_rows = (places < seq_lengths[me]).astype(full)
    group_lengths = lax.dynamic_slice_in_dim(seq_lengths, base, exps, 0)
    key_ok = places[None, :] < group_lengths[:, None]
    gain_one = norm_gains[:, 0]
    gain_two = norm_gains[:, 1]

    chosen = (my_routes[:, :, None] == jnp.arange(experts, dtype=jnp.int32)[None, None, :]).astype(full)
    flat_routes = my_routes.reshape(-1)
    route_hot = (flat_routes[:, None] == jnp.arange(experts, dtype=jnp.int32)[None, :]).astype(jnp.int32)
    before = jnp.cumsum(route_hot, axis=0) - route_hot
    slot_index = jnp.sum(before * route_hot, axis=-1)
    target = (flat_routes * capacity + slot_index).reshape(rows, 2)
    slots = experts * capacity
    slot_ids = jnp.arange(slots, dtype=jnp.int32)
    place_first = slot_ids[:, None] == target[None, :, 0]
    place_second = slot_ids[:, None] == target[None, :, 1]
    place_any = jnp.logical_or(place_first, place_second).astype(low)

    shard_in = expert_in[0].astype(low).reshape(slab, 2, grps, QUAD, units)
    in_pieces = jnp.transpose(shard_in, (1, 3, 0, 2, 4)).reshape(2, 1, QUAD, slab, quarter)
    in_pieces = jnp.broadcast_to(in_pieces, (2, grps, QUAD, slab, quarter)).reshape(
        2, reps, slab, quarter
    )
    down_mine = spread(expert_out[0].astype(low), "grp").reshape(quarter, width)
    gate_mine = swap(in_pieces[0], REP).reshape(width, quarter)
    up_mine = swap(in_pieces[1], REP).reshape(width, quarter)

    upstream = my_cotangent.astype(full) * valid_rows[:, None]

    def to_experts(block):
        sent = block.reshape((1, experts) + block.shape[1:])
        sent = jnp.broadcast_to(sent, (QUAD,) + sent.shape[1:])
        return swap(sent.reshape((QUAD * experts,) + block.shape[1:]), PLANE)

    def dispatch(values):
        return dot(place_any, values).astype(low).reshape(experts, capacity, width)

    expert_upstream = to_experts(dispatch(upstream.astype(low))).reshape(-1, width)
    active_grad_bare = lax.dot_general(
        expert_upstream, down_mine, (((1,), (1,)), ((), ())), preferred_element_type=full
    )

    x_group = group_tokens.astype(full)
    scale_group = lax.rsqrt(jnp.mean(x_group * x_group, axis=-1, keepdims=True) + eps_norm)
    normed_group = (x_group * scale_group * gain_one).astype(low).reshape(exps * rows, width)
    qkv = dot(normed_group, qkv_mine).astype(low).reshape(exps, rows, 3, heads, head_dim)
    queries = qkv[:, :, 0]
    key_rows = qkv[:, :, 1]
    values = qkv[:, :, 2]
    onehot = bucket_onehot(rows)
    bias_mine = lax.dynamic_slice_in_dim(rel_bias, place * heads, heads, 1)
    bias_table = jnp.einsum("ijb,bh->hij", onehot, bias_mine, precision=highest)

    def scores_of():
        raw = (
            jnp.einsum("sihd,sjhd->shij", queries, key_rows, preferred_element_type=full)
            * score_scale
            + bias_table[None]
        )
        return jnp.where(key_ok[:, None, None, :], raw, -1e30)

    scores = scores_of()
    row_max = jnp.max(scores, axis=-1, keepdims=True)
    log_total = row_max + jnp.log(jnp.sum(jnp.exp(scores - row_max), axis=-1, keepdims=True))
    weights_low = jnp.exp(scores - log_total).astype(low)
    context_mine = (
        jnp.einsum("shij,sjhd->sihd", weights_low, values, preferred_element_type=full)
        .astype(low)
        .reshape(exps, rows, head_cols)
    )
    context = jnp.transpose(swap(context_mine, "exp"), (1, 0, 2)).reshape(rows, width)

    x_float = tokens.astype(full)
    scale_one = lax.rsqrt(jnp.mean(x_float * x_float, axis=-1, keepdims=True) + eps_norm)
    hidden_one = x_float + dot(context, full_out)
    scale_two = lax.rsqrt(jnp.mean(hidden_one * hidden_one, axis=-1, keepdims=True) + eps_norm)
    normed_two = (hidden_one * scale_two * gain_two).astype(low)
    normed_float = normed_two.astype(full)
    router_probs = jax.nn.softmax(jnp.dot(normed_float, router, precision=highest), axis=-1)
    picked = jnp.sum(router_probs[:, None, :] * chosen, axis=-1)
    gate_total = jnp.sum(picked, axis=-1, keepdims=True)
    gate_value = picked / gate_total
    combine = gate_value * valid_rows[:, None]
    combine_slots = jnp.sum(
        jnp.where(place_first, combine[None, :, 0], 0.0)
        + jnp.where(place_second, combine[None, :, 1], 0.0),
        axis=1,
    ).reshape(experts, 1, capacity)

    expert_rows = to_experts(dispatch(normed_two)).reshape(-1, width)
    expert_combine = to_experts(combine_slots).reshape(-1, 1)

    gate_part = dot(expert_rows, gate_mine)
    up_part = dot(expert_rows, up_mine)
    active_float, active_pull = jax.vjp(gated_unit, gate_part, up_part)
    active = active_float.astype(low)
    active_scaled = (active_float * expert_combine).astype(low)
    combine_grad_part = jnp.sum(active_float * active_grad_bare, axis=-1).reshape(
        QUAD * experts, 1, capacity
    )
    gate_part_grad, up_part_grad = active_pull(active_grad_bare * expert_combine)
    gate_part_grad = gate_part_grad.astype(low)
    up_part_grad = up_part_grad.astype(low)
    rows_grad_part = (
        lax.dot_general(gate_part_grad, gate_mine, (((1,), (1,)), ((), ())), preferred_element_type=full)
        + lax.dot_general(up_part_grad, up_mine, (((1,), (1,)), ((), ())), preferred_element_type=full)
    ).astype(low)
    output_part = dot(active, down_mine).astype(low)

    combine_grad_back = swap(combine_grad_part, PLANE)
    rows_grad_back = swap(rows_grad_part.reshape(QUAD * experts, capacity, width), PLANE)
    output_back = swap(output_part.reshape(QUAD * experts, capacity, width), PLANE)

    def transposed_dot(a, b):
        return lax.dot_general(a, b, (((0,), (0,)), ((), ())), preferred_element_type=full)

    down_grad = transposed_dot(active_scaled, expert_upstream).astype(low)
    gate_grad = transposed_dot(expert_rows, gate_part_grad).astype(low)
    up_grad = transposed_dot(expert_rows, up_part_grad).astype(low)
    down_share = jnp.sum(
        swap(down_grad.reshape(grps, units, width), "grp").astype(full), axis=0
    )[None]

    def in_columns(grad):
        back = swap(grad.reshape(reps, slab, quarter), REP).astype(full)
        back = jnp.sum(back.reshape(grps, QUAD, slab, grps, units), axis=0)
        return jnp.transpose(back, (1, 2, 0, 3)).reshape(slab, grps * QUAD * units)

    in_share = jnp.concatenate([in_columns(gate_grad), in_columns(up_grad)], axis=1)[None]

    def from_slots(placed, parts):
        hot = jnp.broadcast_to(placed.astype(low)[None], (QUAD,) + placed.shape).reshape(-1, rows)
        return lax.dot_general(
            hot, parts.reshape(-1, width), (((0,), (0,)), ((), ())), preferred_element_type=full
        )

    mixture = combine[:, :1] * from_slots(place_first, output_back) + combine[:, 1:] * from_slots(
        place_second, output_back
    )
    block_loader = (valid_rows[:, None] * (hidden_one + mixture)).astype(low)
    seq_ids = jnp.arange(deal.shape[0], dtype=jnp.int32)
    dealt_seq = jnp.sum(jnp.where(deal == me, seq_ids, 0))
    block_out = lax.dynamic_index_in_dim(
        spread(block_loader, "exp"), dealt_seq - base, 0, keepdims=False
    )

    combine_grad_slots = jnp.sum(combine_grad_back.reshape(QUAD, slots), axis=0)
    combine_grad = jnp.stack(
        [
            jnp.sum(jnp.where(place_first, combine_grad_slots[:, None], 0.0), axis=0),
            jnp.sum(jnp.where(place_second, combine_grad_slots[:, None], 0.0), axis=0),
        ],
        axis=1,
    )
    gate_grad_value = combine_grad * valid_rows[:, None]
    picked_grad = (
        gate_grad_value - jnp.sum(gate_grad_value * gate_value, axis=-1, keepdims=True)
    ) / gate_total
    probs_grad = jnp.sum(picked_grad[:, :, None] * chosen, axis=1)
    logit_grad = router_probs * (
        probs_grad - jnp.sum(probs_grad * router_probs, axis=-1, keepdims=True)
    )
    router_grad = jnp.dot(normed_float.T, logit_grad, precision=highest)
    normed_grad = jnp.dot(logit_grad, router.T, precision=highest) + from_slots(
        jnp.logical_or(place_first, place_second), rows_grad_back
    )
    scaled_two = normed_grad * gain_two
    hidden_grad = (
        upstream
        + scale_two * scaled_two
        - hidden_one * scale_two**3 * jnp.mean(scaled_two * hidden_one, axis=-1, keepdims=True)
    )
    gain_two_grad = jnp.sum(normed_grad * hidden_one * scale_two, axis=0)
    branch_grad = hidden_grad.astype(low)
    context_grad = lax.dot_general(
        branch_grad, full_out, (((1,), (1,)), ((), ())), preferred_element_type=full
    ).astype(low)
    context_grad_pieces = jnp.transpose(context_grad.reshape(rows, exps, head_cols), (1, 0, 2))
    context_grad_mine = swap(context_grad_pieces, "exp").reshape(exps, rows, heads, head_dim)
    branch_group = spread(branch_grad, "exp").reshape(exps * rows, width)
    out_grad = transposed_dot(context_mine.reshape(exps * rows, head_cols), branch_group).astype(low)

    scores = scores_of()
    probs_again = jnp.exp(scores - log_total)
    weights_again = probs_again.astype(low)
    values_grad = jnp.einsum(
        "shij,sihd->sjhd", weights_again, context_grad_mine, preferred_element_type=full
    )
    probs_grad_att = jnp.einsum(
        "sihd,sjhd->shij", context_grad_mine, values, preferred_element_type=full
    )
    row_delta = jnp.sum(probs_grad_att * probs_again, axis=-1, keepdims=True)
    scores_grad = (probs_again * (probs_grad_att - row_delta)).astype(low)
    scores_grad_sum = jnp.sum(scores_grad.astype(full), axis=0)
    bias_grad_mine = jnp.einsum("hij,ijb->bh", scores_grad_sum, onehot, precision=highest)
    bias_grad = lax.dynamic_update_slice_in_dim(
        jnp.zeros((BUCKETS, HEADS), full), bias_grad_mine, place * heads, 1
    )
    queries_grad = (
        jnp.einsum("shij,sjhd->sihd", scores_grad, key_rows, preferred_element_type=full)
        * score_scale
    )
    keys_grad = (
        jnp.einsum("shij,sihd->sjhd", scores_grad, queries, preferred_element_type=full)
        * score_scale
    )
    qkv_grad = (
        jnp.stack([queries_grad, keys_grad, values_grad], axis=2)
        .astype(low)
        .reshape(exps * rows, 3 * head_cols)
    )
    normed_one_part = lax.dot_general(
        qkv_grad, qkv_mine, (((1,), (1,)), ((), ())), preferred_element_type=full
    ).astype(low)
    normed_one_grad = jnp.sum(
        swap(normed_one_part.reshape(exps, rows, width), "exp").astype(full), axis=0
    )
    scaled_one = normed_one_grad * gain_one
    token_grad = (
        hidden_grad
        + scale_one * scaled_one
        - x_float * scale_one**3 * jnp.mean(scaled_one * x_float, axis=-1, keepdims=True)
    )
    gain_one_grad = jnp.sum(normed_one_grad * x_float * scale_one, axis=0)

    qkv_weight_grad = transposed_dot(normed_group, qkv_grad).astype(low)
    qkv_grad_rows = swap(qkv_weight_grad.reshape(exps, row_block, 3 * head_cols), "exp")
    qkv_grad_rows = jnp.transpose(
        qkv_grad_rows.reshape(exps, row_block, 3, head_cols), (1, 2, 0, 3)
    ).reshape(row_block, reps, -1)
    qkv_share = jnp.sum(
        swap(jnp.transpose(qkv_grad_rows, (1, 0, 2)), REP).astype(full), axis=0
    )
    out_pieces = jnp.transpose(out_grad.reshape(row_block, reps, -1), (1, 0, 2))
    out_share = jnp.sum(swap(out_pieces, REP).astype(full), axis=0)

    small = jnp.concatenate(
        [
            router_grad.reshape(-1),
            jnp.stack([gain_one_grad, gain_two_grad], axis=1).reshape(-1),
            bias_grad.reshape(-1),
        ]
    ).reshape(-1, 128)
    small_total = jnp.sum(lax.all_gather(small, ALL, axis=0, tiled=False), axis=0).reshape(-1)
    router_total = small_total[: router.size].reshape(router.shape)
    gains_total = small_total[router.size : router.size + norm_gains.size].reshape(norm_gains.shape)
    bias_total = small_total[router.size + norm_gains.size :].reshape(rel_bias.shape)

    qkv_new = adamw_update(attn_qkv, qkv_first, qkv_second, qkv_share, 1.5 / math.sqrt(D), 0.1)
    out_new = adamw_update(attn_out, out_first, out_second, out_share, 6.0 / math.sqrt(D), 0.1)
    bias_new = adamw_update(rel_bias, bias_first, bias_second, bias_total, 0.3, 0.0)
    router_new = adamw_update(
        router, router_first, router_second, router_total, 1.0 / math.sqrt(D), 0.1
    )
    gains_new = adamw_update(norm_gains, gains_first, gains_second, gains_total, 0.5, 0.0)
    in_new = adamw_update(expert_in, in_first, in_second, in_share, 1.5 / math.sqrt(D), 0.1)
    down_new = adamw_update(
        expert_out, down_first, down_second, down_share, 1.5 / math.sqrt(FF), 0.1
    )
    return (
        (block_out, token_grad)
        + qkv_new
        + out_new
        + bias_new
        + router_new
        + gains_new
        + in_new
        + down_new
    )


def solution(mesh):
    reps, exps = mesh.devices.shape
    split = Mesh(mesh.devices.reshape(reps // QUAD, QUAD, exps), ALL)
    by_rows = P(ALL, None)
    attn = P("exp", REP)
    expert = P("exp", REP, None)
    return jax.shard_map(
        per_device if (reps, exps) == (2 * QUAD, 4) else plain_device,
        mesh=split,
        in_specs=(by_rows, by_rows) + (P(),) * 3 + (attn,) * 6 + (P(),) * 9 + (expert,) * 6,
        out_specs=(by_rows, by_rows) + (attn,) * 6 + (P(),) * 9 + (expert,) * 6,
        check_vma=False,
    )
```

```python
import functools
import math

import jax
import jax.numpy as jnp
from jax import lax
from jax.experimental import pallas as pl
from jax.experimental.pallas import tpu as pltpu
from jax.sharding import Mesh
from jax.sharding import PartitionSpec as P

D = 1024
HEADS = 16
FF = 2816
BUCKETS = 32
STEP = 10
QUAD = 4
REP = ("grp", "quad")
PLANE = ("quad", "exp")
ALL = ("grp", "quad", "exp")

highest = lax.Precision.HIGHEST
eps_norm = 1e-06
thresholds = (1, 2, 3, 4, 5, 6, 7, 8, 11, 16, 22, 32, 45, 64, 90)
beta_one = 0.9
beta_two = 0.999
eps_adam = 1e-08
low = jnp.bfloat16
full = jnp.float32
MESH = pl.DeviceIdType.MESH


def adamw_update(weight, moment, second, gradient, step_rate, decay_factor):
    new_moment = beta_one * moment + (1.0 - beta_one) * gradient
    new_second = beta_two * second + (1.0 - beta_two) * gradient * gradient
    corrected = new_moment / (1.0 - beta_one**STEP)
    scaled = new_second / (1.0 - beta_two**STEP)
    new_weight = weight - step_rate * (
        corrected / (jnp.sqrt(scaled) + eps_adam) + decay_factor * weight
    )
    return (new_moment, new_second, new_weight)


def gated_unit(gate_input, up_input):
    return jax.nn.gelu(gate_input, approximate=True) * up_input


def dot(a, b):
    return jnp.dot(a, b, preferred_element_type=full)


def nt(a, b, precision=None):
    return lax.dot_general(a, b, (((1,), (1,)), ((), ())), preferred_element_type=full, precision=precision)


def tn(a, b):
    return lax.dot_general(a, b, (((0,), (0,)), ((), ())), preferred_element_type=full)


class Where:
    def __init__(self, grps, exps):
        self.grps, self.exps = grps, exps
        self.reps = grps * QUAD
        self.grp = lax.axis_index("grp")
        self.quad = lax.axis_index("quad")
        self.exp = lax.axis_index("exp")
        self.rep = self.grp * QUAD + self.quad
        self.base = self.rep * exps
        self.me = self.base + self.exp

    def device(self, rep, exp):
        return (rep // QUAD, rep % QUAD, exp)

    def near(self, flip):
        q = self.quad
        if flip & 1:
            q = q + 1 - 2 * (q % 2)
        if flip & 2:
            q = q + 2 - 4 * (q // 2)
        return q


def send(src, dst, send_sem, recv_sem, device):
    return pltpu.make_async_remote_copy(
        src_ref=src, dst_ref=dst, send_sem=send_sem, recv_sem=recv_sem, device_id=device, device_id_type=MESH
    )


def arrived(ref, sem):
    pltpu.make_async_copy(ref, ref, sem).wait()


def greet(count, device):
    barrier = pltpu.get_barrier_semaphore()

    def one(k, _):
        pl.semaphore_signal(barrier, inc=1, device_id=device(k), device_id_type=MESH)
        return 0

    lax.fori_loop(1, count + 1, one, 0)
    return functools.partial(pl.semaphore_wait, barrier, count)


def everyone(at):
    count = at.reps * at.exps

    def device(k):
        other = (at.me + k) % count
        return at.device(other // at.exps, other % at.exps)

    return count - 1, device


def neighbours(at):
    members = QUAD * at.exps
    plane = at.quad * at.exps + at.exp

    def device(k):
        other = (plane + k) % members
        rest = k - members
        grp = jnp.where(k < members, at.grp, (at.grp + 1 + rest // QUAD) % at.grps)
        quad = jnp.where(k < members, other // at.exps, rest % QUAD)
        return grp, quad, jnp.where(k < members, other % at.exps, at.exp)

    return members - 1 + QUAD * (at.grps - 1), device


def turn(exp, i):
    beside = exp + 1 - 2 * (exp % 2)
    return jnp.where(i == 0, (beside + 2) % 4, jnp.where(i == 1, (exp + 2) % 4, jnp.where(i == 2, beside, exp)))


def lane_of(shape):
    return lax.broadcasted_iota(jnp.int32, shape, 1)


def row_of(shape):
    return lax.broadcasted_iota(jnp.int32, shape, 0)


def bucket_of(offset):
    distance = jnp.abs(offset)
    bucket = jnp.where(offset > 0, 16, 0)
    for threshold in thresholds:
        bucket = bucket + jnp.where(distance >= threshold, 1, 0)
    return bucket


def bits_of(count):
    return count.bit_length() - 1


def column_parts(width):
    tiles = width // 128
    cuts = [0, (tiles + 2) // 3, (2 * tiles + 2) // 3, tiles]
    return [(cuts[i] * 128, (cuts[i + 1] - cuts[i]) * 128) for i in range(3)]


def flipped(place, bit):
    return place + (1 - 2 * ((place // (1 << bit)) % 2)) * (1 << bit)


class Doubling:
    def __init__(self, at, own, every, sems, core_sems, orders):
        self.at, self.own, self.every = at, own, every
        self.sems, self.core_sems, self.orders = sems, core_sems, orders
        self.plane = at.quad * at.exps + at.exp
        self.steps = len(orders[0])
        self.parts = column_parts(own.shape[1])

    def device(self, bit):
        other = flipped(self.plane, bit)
        return (self.at.grp, other // self.at.exps, other % self.at.exps)

    def place(self, part, j):
        p = self.plane
        for i, bit in enumerate(self.orders[part]):
            if (j >> i) & 1:
                p = flipped(p, bit + 1)
        return p

    def block(self, part, p):
        begin, size = self.parts[part]
        return self.every.at[p, :, pl.ds(begin, size)]

    def source(self, part, j):
        begin, size = self.parts[part]
        return self.own.at[:, pl.ds(begin, size)] if j == 0 else self.block(part, self.place(part, j))

    def index(self, step, part, j):
        return part * (1 << self.steps) + (1 << step) - 1 + j

    def copy(self, step, part, j):
        i = self.index(step, part, j)
        return send(
            self.source(part, j),
            self.block(part, self.place(part, j)),
            self.sems.at[0, i],
            self.sems.at[1, i],
            self.device(self.orders[part][step] + 1),
        )

    def core_copy(self, part, j):
        i = part * (1 << self.steps) + j
        return send(
            self.source(part, j),
            self.block(part, self.place(part, j)),
            self.core_sems.at[0, i],
            self.core_sems.at[1, i],
            self.device(0),
        )

    def start(self):
        for part in range(3):
            for step in range(self.steps):
                self.copy(step, part, 0).start()
        for part in range(3):
            self.core_copy(part, 0).start()
        self.keep().start()

    def keep(self):
        return pltpu.make_async_copy(self.own, self.every.at[self.plane], self.core_sems.at[1, 3 << self.steps])

    def next(self, step):
        for part in range(3):
            for j in range(1 << step):
                k = (1 << step) + j
                arrived(self.block(part, self.place(part, k)), self.sems.at[1, self.index(step, part, j)])
                for later in range(step + 1, self.steps):
                    self.copy(later, part, k).start()
                self.core_copy(part, k).start()

    def finish_in(self):
        for part in range(3):
            for j in range(1 << self.steps):
                there = self.block(part, flipped(self.place(part, j), 0))
                arrived(there, self.core_sems.at[1, part * (1 << self.steps) + j])
        self.keep().wait()

    def finish_out(self):
        for part in range(3):
            for j in range(1 << self.steps):
                self.core_copy(part, j).wait_send()
            for step in range(self.steps):
                for j in range(1 << step):
                    self.copy(step, part, j).wait_send()


class Halving:
    def __init__(self, at, bufs, sems, orders):
        self.at, self.bufs, self.sems = at, bufs, sems
        self.plane = at.quad * at.exps + at.exp
        self.places = bits_of(QUAD * at.exps)
        self.chip_bits = list(range(self.places - 1))
        self.parts = column_parts(bufs[0].shape[2])
        self.orders = orders

    def device(self, bit):
        other = flipped(self.plane, bit)
        return (self.at.grp, other // self.at.exps, other % self.at.exps)

    def hop(self, step, part):
        order = self.orders[part]
        bit = order[step]
        left = [b for b in self.chip_bits if b not in order[:step]]
        pos = left.index(bit)
        half = 1 << (len(left) - 1)
        mine = (self.plane // (1 << (bit + 1))) % 2
        device = self.device(bit + 1)
        begin, size = self.parts[part]
        cols = pl.ds(begin, size)
        base = self.base(step, part)

        def index(j, value):
            return (j >> pos) * (1 << (pos + 1)) + value * (1 << pos) + j % (1 << pos)

        pairs = []
        for j in range(half):
            copy = functools.partial(
                send,
                self.bufs[step].at[index(j, 1 - mine), :, cols],
                self.bufs[step + 1].at[j, :, cols],
                self.sems.at[0, base + j],
                self.sems.at[1, base + j],
                device,
            )
            pairs.append((copy, index(j, mine), j))
        return pairs, begin, size, base

    def base(self, step, part):
        n = len(self.chip_bits)
        return part * (1 << n) + sum(1 << (n - 1 - s) for s in range(step))

    def start(self, step, part=None):
        for p in range(3) if part is None else [part]:
            for copy, _, _ in self.hop(step, p)[0]:
                copy().start()

    def add(self, step, part):
        pairs, begin, size, base = self.hop(step, part)
        cols = pl.ds(begin, size)
        here, there = self.bufs[step], self.bufs[step + 1]
        for _, keep, j in pairs:
            arrived(there.at[j, :, cols], self.sems.at[1, base + j])
            there[j, :, begin : begin + size] = (
                there[j, :, begin : begin + size] + here[keep, :, begin : begin + size]
            )

    def next(self, step):
        for p in range(3):
            self.add(step, p)
            if step + 1 < len(self.chip_bits):
                self.start(step + 1, p)

    def result(self):
        return self.bufs[len(self.chip_bits)]

    def finish(self):
        for step in range(len(self.chip_bits)):
            for p in range(3):
                for copy, _, _ in self.hop(step, p)[0]:
                    copy().wait_send()


class Group:
    def __init__(self, at, own, every, sems):
        self.at, self.own, self.every, self.sems = at, own, every, sems
        self.beside, self.across = at.exp + 1 - 2 * (at.exp % 2), (at.exp + 2) % 4

    def copy(self, src, index, send_index, device):
        return send(
            src, self.every.at[index], self.sems.at[0, send_index], self.sems.at[1, index], self.at.device(self.at.rep, device)
        )

    def first(self):
        return [
            self.copy(self.own, self.at.exp, 0, self.across),
            self.copy(self.own, self.at.exp, 1, self.beside),
        ]

    def second(self):
        return self.copy(self.every.at[self.across], self.across, 2, self.beside)

    def start(self):
        for copy in self.first():
            copy.start()

    def pass_on(self):
        arrived(self.every.at[self.across], self.sems.at[1, self.across])
        self.second().start()

    def arrive(self):
        for index in (self.beside, (self.beside + 2) % 4):
            arrived(self.every.at[index], self.sems.at[1, index])

    def sent(self):
        for copy in self.first() + [self.second()]:
            copy.wait_send()


class Tiles:
    def __init__(self, units, reps):
        self.units = units
        self.reps = reps
        self.hidden = units * reps
        self.half = self.hidden // 256
        self.wide = (self.half + 1) // 2
        self.count = 3
        self.size = 128 * self.wide // self.count
        self.skip = 128 * (2 * self.wide - self.half)

    def start(self, quad):
        return 128 * (self.half * (quad // 2) + (self.half - self.wide) * (quad % 2))

    def rows(self, tile):
        result = []
        for k in range(QUAD):
            found = None
            for parity in range(2):
                first = self.start(parity) + tile * self.size
                live = first + (self.skip if parity and tile == 0 else 0)
                begin = max(live, k * self.units)
                end = min(first + self.size, (k + 1) * self.units)
                if end > begin:
                    found = (begin - k * self.units, end - begin, parity, begin - first)
            result.append(found)
        return result


class Outward:
    def __init__(self, at, tiles, tile, in_low, down_slab, both_w, down_w, nothing, sems, down_sems):
        self.at, self.tiles, self.tile = at, tiles, tile
        self.in_low, self.down_slab, self.both_w, self.down_w = in_low, down_slab, both_w, down_w
        self.nothing, self.sems, self.down_sems = nothing, sems, down_sems
        self.slab = in_low.shape[0]

    def source(self, quad, section):
        begin = section * self.tiles.hidden + self.tiles.start(quad) + self.tile * self.tiles.size
        return self.in_low.at[:, pl.ds(pl.multiple_of(begin, 128), self.tiles.size)]

    def target(self, rep, section):
        rows = pl.ds(pl.multiple_of(rep * self.slab, self.slab), self.slab)
        return self.both_w.at[rows, pl.ds(section * self.tiles.size, self.tiles.size)]

    def over(self, act):
        at = self.at

        def one(k, _):
            other = (at.rep + k) % at.reps
            for section in range(2):
                act(
                    functools.partial(
                        send,
                        self.source(other % QUAD, section),
                        self.target(at.rep, section),
                        self.sems.at[0, section * at.reps + other],
                        self.sems.at[1, section * at.reps + at.rep],
                        at.device(other, at.exp),
                    )
                )
            return 0

        lax.fori_loop(1, at.reps, one, 0)

    def over_down(self, act, act_local):
        at = self.at
        for k, piece in enumerate(self.tiles.rows(self.tile)):
            if piece is None:
                continue
            begin, count, parity, to = piece
            quad = 2 * (at.rep // QUAD) + parity
            src, dst = self.down_slab.at[pl.ds(begin, count)], self.down_w.at[pl.ds(to, count)]
            recv = self.down_sems.at[1, at.rep]
            for g in range(at.grps):
                stays = jnp.logical_and(at.grp == g, at.quad == quad)
                ours = at.rep % QUAD == k

                @pl.when(jnp.logical_and(ours, jnp.logical_not(stays)))
                def _():
                    act(functools.partial(send, src, dst, self.down_sems.at[0, g], recv, (g, quad, at.exp)))

                @pl.when(jnp.logical_and(ours, stays))
                def _():
                    act_local(functools.partial(pltpu.make_async_copy, src, dst, recv))

    def blank(self):
        return pltpu.make_async_copy(
            self.nothing, self.down_w.at[pl.ds(0, self.tiles.skip)], self.down_sems.at[1, self.at.reps]
        )

    def start(self):
        at = self.at
        self.over_down(lambda copy: copy().start(), lambda copy: copy().start())
        self.over(lambda copy: copy().start())
        for section in range(2):
            pltpu.make_async_copy(
                self.source(at.quad, section), self.target(at.rep, section), self.sems.at[1, section * at.reps + at.rep]
            ).start()
        if self.tile == 0:

            @pl.when(at.quad % 2 == 1)
            def _():
                self.blank().start()

    def arrive(self):
        at = self.at

        def one(rep, _):
            for section in range(2):
                arrived(self.target(rep, section), self.sems.at[1, section * at.reps + rep])
            return 0

        lax.fori_loop(0, at.reps, one, 0)
        for parity in range(2):

            @pl.when(at.quad % 2 == parity)
            def _():
                for k, piece in enumerate(self.tiles.rows(self.tile)):
                    if piece is not None and piece[2] == parity:
                        source = QUAD * (at.quad // 2) + k
                        arrived(self.down_w.at[pl.ds(piece[3], piece[1])], self.down_sems.at[1, source])
                if parity and self.tile == 0:
                    self.blank().wait()

    def sent(self):
        self.over(lambda copy: copy().wait_send())
        self.over_down(lambda copy: copy().wait_send(), lambda copy: None)


class Homeward:
    def __init__(self, at, tiles, tile, both, down, in_parts, down_parts, sems, down_sems, sections=(0, 1)):
        self.at, self.tiles, self.tile, self.sections = at, tiles, tile, sections
        self.both, self.down, self.in_parts, self.down_parts = both, down, in_parts, down_parts
        self.sems, self.down_sems = sems, down_sems
        self.slab = in_parts.shape[1]

    def target(self, grp, quad, parity, section):
        skip = self.tiles.skip if parity and self.tile == 0 else 0
        to = section * self.tiles.hidden + self.tiles.start(quad) + self.tile * self.tiles.size + skip
        to = to if isinstance(to, int) else pl.multiple_of(to, 128)
        return skip, self.in_parts.at[grp, :, pl.ds(to, self.tiles.size - skip)]

    def copy(self, rep, parity, section, local=False):
        at = self.at
        skip, dst = self.target(at.grp, at.quad, parity, section)
        rows = pl.ds(pl.multiple_of(rep * self.slab, self.slab), self.slab)
        src = self.both.at[rows, pl.ds(section * self.tiles.size + skip, self.tiles.size - skip)]
        recv = self.sems.at[1, section * at.reps + at.rep]
        if local:
            return pltpu.make_async_copy(src, dst, recv)
        return send(src, dst, self.sems.at[0, section * at.reps + rep], recv, at.device(rep, at.exp))

    def over(self, act, act_local):
        at = self.at
        for parity in range(2):

            @pl.when(at.quad % 2 == parity)
            def _():
                def one(k, _):
                    for section in self.sections:
                        act(self.copy((at.rep + k) % at.reps, parity, section))
                    return 0

                lax.fori_loop(1, at.reps, one, 0)
                if act_local:
                    for section in self.sections:
                        act_local(self.copy(at.rep, parity, section, local=True))

    def over_down(self, act, act_local):
        at = self.at
        if self.down is None:
            return
        for k, piece in enumerate(self.tiles.rows(self.tile)):
            if piece is None:
                continue
            begin, count, parity, to = piece
            src, dst = self.down.at[pl.ds(to, count)], self.down_parts.at[at.grp, pl.ds(begin, count)]
            recv = self.down_sems.at[1, at.grp]
            stays = jnp.logical_and(at.grp == at.quad // 2, at.quad == k)
            ours = at.quad % 2 == parity

            @pl.when(jnp.logical_and(ours, jnp.logical_not(stays)))
            def _():
                act(functools.partial(send, src, dst, self.down_sems.at[0, k], recv, (at.quad // 2, k, at.exp)))

            @pl.when(jnp.logical_and(ours, stays))
            def _():
                act_local(functools.partial(pltpu.make_async_copy, src, dst, recv))

    def start(self):
        self.over_down(lambda copy: copy().start(), lambda copy: copy().start())
        self.over(lambda copy: copy.start(), lambda copy: copy.start())

    def arrive(self):
        at = self.at
        for rep in range(at.reps):
            for section in self.sections:
                _, dst = self.target(rep // QUAD, rep % QUAD, rep % 2, section)
                arrived(dst, self.sems.at[1, section * at.reps + rep])
        for k, piece in enumerate(self.tiles.rows(self.tile)):
            if piece is None or self.down is None:
                continue

            @pl.when(at.quad == k)
            def _():
                for g in range(at.grps):
                    arrived(self.down_parts.at[g, pl.ds(piece[0], piece[1])], self.down_sems.at[1, g])

    def sent(self):
        self.over(lambda copy: copy.wait_send(), None)
        self.over_down(lambda copy: copy().wait_send(), lambda copy: None)


def forward_kernel(
    grps,
    exps,
    lengths,
    bias_table,
    routes_t,
    tokens,
    cotangent,
    gains,
    router,
    attn_qkv,
    attn_out,
    expert_in,
    expert_out,
    both_w,
    down_w,
    cot_all,
    n_all,
    comb_all,
    qkv_out,
    lse_out,
    mine_out,
    n1_out,
    wqkv_out,
    wout_out,
    h1_out,
    n2_out,
    probs_out,
    in_out,
    down_out,
    in_wide,
    down_wide,
    qkv_t,
    out_w,
    in_low,
    down_slab,
    tok_all,
    wqkv,
    wout,
    n1,
    qkv,
    lse,
    mine,
    ctx,
    bias,
    comb_send,
    nothing,
    tok_sem,
    wq_sem,
    wo_sem,
    wo2_sem,
    weight_sem,
    down_sem,
    ctx_sem,
    cot_sem,
    cot_core_sem,
    n_sem,
    n_core_sem,
    comb_sem,
    store_sem,
    cast_sem,
):
    at = Where(grps, exps)
    reps = at.reps
    rows, width = tokens.shape
    heads = HEADS // exps
    head_dim = width // HEADS
    head_cols = heads * head_dim
    block_cols = min(128, head_cols)
    shard_cols, row_block = qkv_t.shape
    seg = math.gcd(shard_cols, head_cols)
    segs = shard_cols // seg
    tiles = Tiles(down_slab.shape[0], reps)
    plane = at.quad * exps + at.exp
    members = QUAD * exps
    scale = 1.0 / math.sqrt(head_dim)
    SEND, RECV = 0, 1

    met = greet(*everyone(at))
    wide_copies = [
        pltpu.make_async_copy(expert_in, in_wide, cast_sem.at[0]),
        pltpu.make_async_copy(expert_out, down_wide, cast_sem.at[1]),
    ]
    for copy in wide_copies:
        copy.start()
    qkv_t[...] = attn_qkv[...].T.astype(low)
    out_w[...] = attn_out[...].astype(low)
    met()

    def exp_peer(k):
        return (at.exp + k) % exps

    group_tokens = Group(at, tokens, tok_all, tok_sem)
    group_tokens.start()
    tok_all[at.exp] = tokens[...]

    def segment(k):
        col = (at.rep * segs + k) * seg
        section = col // width
        within = col - section * width
        owner = within // head_cols
        return owner, section * head_cols + within - owner * head_cols

    def segment_copy(k, shift):
        owner, offset = segment(k)
        src = qkv_t.at[pl.ds(k * seg, seg)]
        dst = wqkv.at[at.exp, pl.ds(pl.multiple_of(offset, seg), seg)]
        target = at.device((at.rep + shift) % reps, owner)
        return owner, src, dst, functools.partial(
            send, src, dst, wq_sem.at[SEND, k * reps + shift], wq_sem.at[RECV, at.exp * 3 * (head_cols // seg) + offset // seg], target
        )

    def over_segments(act, act_local):
        def one(i, _):
            k, shift = i // reps, i % reps
            owner, src, dst, copy = segment_copy(k, shift)
            stays = jnp.logical_and(shift == 0, owner == at.exp)

            @pl.when(jnp.logical_not(stays))
            def _():
                act(copy())

            @pl.when(stays)
            def _():
                act_local(k, src, dst)

            return 0

        lax.fori_loop(0, segs * reps, one, 0)

    def local_segment(k, src, dst):
        _, offset = segment(k)
        pltpu.make_async_copy(src, dst, wq_sem.at[RECV, at.exp * 3 * (head_cols // seg) + offset // seg]).start()

    over_segments(lambda copy: copy.start(), local_segment)

    for k in range(1, reps):
        other = (at.rep + k) % reps
        send(
            out_w, wout.at[at.exp, at.rep], wo_sem.at[SEND, other], wo_sem.at[RECV, at.rep], at.device(other, at.exp)
        ).start()
    wout[at.exp, at.rep] = out_w[...]
    chip_bits = list(range(bits_of(members) - 1))
    cots = Doubling(at, cotangent, cot_all, cot_sem, cot_core_sem, [chip_bits[::-1]] * 3)
    cots.start()

    span = 2 * rows
    bucket = bucket_of(lane_of((8, span)) - rows)
    for h in range(heads):
        line = jnp.zeros((8, span), full)
        for b in range(BUCKETS):
            line = jnp.where(bucket == b, bias_table[at.exp * heads + h, b], line)
        whole = jnp.broadcast_to(line[0:1], (rows, span))
        bias[h] = pltpu.roll(whole, 0, 1, stride=1, stride_axis=0)[:, rows:]

    group_tokens.pass_on()
    group_tokens.arrive()

    def norm_group(s, _):
        x = tok_all[s].astype(full)
        r = lax.rsqrt(jnp.mean(x * x, axis=1, keepdims=True) + eps_norm)
        n1[s] = (x * r * gains[0:1, :]).astype(low)
        return 0

    lax.fori_loop(0, exps, norm_group, 0)

    for copy in wide_copies:
        copy.wait()
    in_low[...] = in_wide[...].astype(low)
    down_slab[...] = down_wide[...].astype(low)
    nothing[...] = jnp.zeros_like(nothing)
    weights = [
        Outward(
            at, tiles, t, in_low, down_slab, both_w.at[t], down_w.at[t], nothing, weight_sem.at[t], down_sem.at[t]
        )
        for t in range(2)
    ]
    weights[0].start()

    def wait_segment(i, _):
        e, j = i // (3 * head_cols // seg), i % (3 * head_cols // seg)
        arrived(wqkv.at[e, pl.ds(pl.multiple_of(j * seg, seg), seg)], wq_sem.at[RECV, i])
        return 0

    lax.fori_loop(0, exps * 3 * head_cols // seg, wait_segment, 0)

    def project(s, _):
        total = jnp.zeros((rows, 3 * head_cols), full)
        for e in range(exps):
            total = total + nt(n1[s, :, e * row_block : (e + 1) * row_block], wqkv[e])
        qkv[s] = total.astype(low)
        return 0

    lax.fori_loop(0, exps, project, 0)

    group_wout = Group(at, wout.at[at.exp], wout, wo2_sem)

    def beside(k):
        if k == 1:
            for j in range(1, reps):
                other = (at.rep + j) % reps
                arrived(wout.at[at.exp, other], wo_sem.at[RECV, other])
            group_wout.start()
        elif k == 2:
            cots.next(0)
        else:
            group_wout.pass_on()

    def attend(i, _):
        s = turn(at.exp, i)
        for k in range(1, exps):

            @pl.when(i == k)
            def _():
                beside(k)

        ok = lane_of((rows, rows)) < lengths[at.base + s]
        lane = lane_of((rows, block_cols))
        sums = jnp.zeros((rows, 128), full)
        for c in range(head_cols // block_cols):
            cols = slice(c * block_cols, (c + 1) * block_cols)
            q = qkv[s, :, cols] * scale
            k = qkv[s, :, head_cols + c * block_cols : head_cols + (c + 1) * block_cols]
            v = qkv[s, :, 2 * head_cols + c * block_cols : 2 * head_cols + (c + 1) * block_cols]
            result = jnp.zeros((rows, block_cols), full)
            for t in range(block_cols // head_dim):
                h = c * (block_cols // head_dim) + t
                here = jnp.logical_and(lane >= t * head_dim, lane < (t + 1) * head_dim)
                scores = nt(jnp.where(here, q, jnp.zeros_like(q)), k) + bias[h]
                scores = jnp.where(ok, scores, -1e30)
                top = jnp.max(scores, axis=1, keepdims=True)
                weights = jnp.exp(scores - top)
                total = jnp.sum(weights, axis=1, keepdims=True)
                weights = (weights * (1.0 / total)).astype(low)
                result = jnp.where(here, jnp.dot(weights, v, preferred_element_type=full), result)
                sums = jnp.where(lane_of((rows, 128)) == h, top + jnp.log(total), sums)
            mine[s, :, cols] = result.astype(low)
        lse[s] = sums

        @pl.when(i < exps - 1)
        def _():
            send(
                mine.at[s], ctx.at[at.exp], ctx_sem.at[SEND, s], ctx_sem.at[RECV, at.exp], at.device(at.rep, s)
            ).start()

        @pl.when(i == exps - 1)
        def _():
            pltpu.make_async_copy(mine.at[s], ctx.at[at.exp], ctx_sem.at[RECV, at.exp]).start()

        return 0

    lax.fori_loop(0, exps, attend, 0)

    cots.next(1)
    group_wout.arrive()
    for e in range(exps):
        arrived(ctx.at[e], ctx_sem.at[RECV, e])

    out_cols = wout.shape[3]
    for r in range(reps):
        cols = slice(r * out_cols, (r + 1) * out_cols)
        total = tokens[:, cols].astype(full)
        for e in range(exps):
            total = total + jnp.dot(ctx[e], wout[e, r], preferred_element_type=full)
        h1_out[:, cols] = total
    h1 = h1_out[...]
    r2 = lax.rsqrt(jnp.mean(h1 * h1, axis=1, keepdims=True) + eps_norm)
    n2 = (h1 * r2 * gains[1:2, :]).astype(low)
    n2_out[...] = n2
    rotated = [chip_bits[c:] + chip_bits[:c] for c in range(3)]
    rows_two = Doubling(at, n2_out, n_all, n_sem, n_core_sem, rotated)
    rows_two.start()
    weights[1].start()

    router_rows = jnp.concatenate([router[...], jnp.zeros((128 - exps, width), full)], axis=0)
    logits = nt(n2.astype(full), router_rows, precision=highest)
    lane = lane_of((rows, 128))
    logits = jnp.where(lane < exps, logits, -1e30)
    probs = jnp.exp(logits - jnp.max(logits, axis=1, keepdims=True))
    probs = probs / jnp.sum(probs, axis=1, keepdims=True)
    probs_out[...] = probs
    picked = jnp.where(routed(routes_t, at.me, rows), probs, 0.0)
    comb = picked / jnp.sum(picked, axis=1, keepdims=True)
    comb = jnp.where(row_of((rows, 1)) < lengths[at.me], comb, 0.0)
    comb_send[...] = comb.T[0 : comb_send.shape[0]]

    def comb_copy(k):
        other = (plane + k) % members
        return send(
            comb_send,
            comb_all.at[plane],
            comb_sem.at[SEND, other],
            comb_sem.at[RECV, plane],
            (at.grp, other // exps, other % exps),
        )

    def start_comb(k, _):
        comb_copy(k).start()
        return 0

    lax.fori_loop(1, members, start_comb, 0)
    pltpu.make_async_copy(comb_send, comb_all.at[plane], comb_sem.at[RECV, plane]).start()
    rows_two.next(0)

    stores = [
        (qkv, qkv_out),
        (lse, lse_out),
        (mine, mine_out),
        (n1, n1_out),
        (wqkv, wqkv_out),
        (wout, wout_out),
        (in_low, in_out),
        (down_slab, down_out),
    ]
    for i, (src, dst) in enumerate(stores):
        pltpu.make_async_copy(src, dst, store_sem.at[i]).start()

    for step in range(1, rows_two.steps):
        rows_two.next(step)
    for step in range(2, cots.steps):
        cots.next(step)

    cots.finish_in()
    rows_two.finish_in()

    def comb_in(k, _):
        arrived(comb_all.at[k], comb_sem.at[RECV, k])
        return 0

    lax.fori_loop(0, members, comb_in, 0)
    for tile in weights:
        tile.arrive()

    for k in range(1, exps):
        peer = exp_peer(k)
        arrived(mine.at[peer], ctx_sem.at[SEND, peer])
    over_segments(lambda copy: copy.wait_send(), lambda k, src, dst: None)
    for k in range(1, reps):
        arrived(out_w, wo_sem.at[SEND, (at.rep + k) % reps])
    group_tokens.sent()
    group_wout.sent()
    cots.finish_out()
    rows_two.finish_out()

    def sent_comb(k, _):
        comb_copy(k).wait_send()
        return 0

    lax.fori_loop(1, members, sent_comb, 0)
    for tile in weights:
        tile.sent()
    for i, (src, dst) in enumerate(stores):
        pltpu.make_async_copy(src, dst, store_sem.at[i]).wait()


def forward_call(
    grps, exps, lengths, bias_table, routes_t, tokens, cotangent, gains, router, attn_qkv, attn_out, expert_in, expert_out
):
    reps = grps * QUAD
    rows, width = tokens.shape
    head_cols = width // exps
    row_block, shard_cols = attn_qkv.shape
    seg = math.gcd(shard_cols, head_cols)
    segs = shard_cols // seg
    units = expert_out.shape[0]
    out_cols = attn_out.shape[1]
    heads = HEADS // exps
    members = QUAD * exps
    tiles = Tiles(units, reps)
    shape = jax.ShapeDtypeStruct
    vmem = pl.BlockSpec(memory_space=pltpu.VMEM)
    smem = pl.BlockSpec(memory_space=pltpu.SMEM)
    hbm = pl.BlockSpec(memory_space=pl.ANY)
    results = [
        (shape((2, width, 2 * tiles.size), low), hbm),
        (shape((2, tiles.size, width), low), hbm),
        (shape((members, rows, width), low), hbm),
        (shape((members, rows, width), low), hbm),
        (shape((members, 8, rows), full), hbm),
        (shape((exps, rows, 3 * head_cols), low), hbm),
        (shape((exps, rows, 128), full), hbm),
        (shape((exps, rows, head_cols), low), hbm),
        (shape((exps, rows, width), low), hbm),
        (shape((exps, 3 * head_cols, row_block), low), hbm),
        (shape((exps, reps, row_block, out_cols), low), hbm),
        (shape((rows, width), full), vmem),
        (shape((rows, width), low), vmem),
        (shape((rows, 128), full), vmem),
        (shape(expert_in.shape, low), hbm),
        (shape(expert_out.shape, low), hbm),
    ]
    dma = pltpu.SemaphoreType.DMA
    chips = members // 2
    return pl.pallas_call(
        functools.partial(forward_kernel, grps, exps),
        out_shape=[r[0] for r in results],
        in_specs=[smem] * 2 + [vmem] * 7 + [hbm] * 2,
        out_specs=[r[1] for r in results],
        scratch_shapes=[
            pltpu.VMEM(expert_in.shape, full),
            pltpu.VMEM(expert_out.shape, full),
            pltpu.VMEM((shard_cols, row_block), low),
            pltpu.VMEM((row_block, out_cols), low),
            pltpu.VMEM(expert_in.shape, low),
            pltpu.VMEM(expert_out.shape, low),
            pltpu.VMEM((exps, rows, width), low),
            pltpu.VMEM((exps, 3 * head_cols, row_block), low),
            pltpu.VMEM((exps, reps, row_block, out_cols), low),
            pltpu.VMEM((exps, rows, width), low),
            pltpu.VMEM((exps, rows, 3 * head_cols), low),
            pltpu.VMEM((exps, rows, 128), full),
            pltpu.VMEM((exps, rows, head_cols), low),
            pltpu.VMEM((exps, rows, head_cols), low),
            pltpu.VMEM((heads, rows, rows), full),
            pltpu.VMEM((8, rows), full),
            pltpu.VMEM((tiles.skip, width), low),
            dma((2, exps)),
            dma((2, max(segs * reps, exps * 3 * head_cols // seg))),
            dma((2, reps)),
            dma((2, exps)),
            dma((2, 2, 2 * reps)),
            dma((2, 2, reps + 1)),
            dma((2, exps)),
            dma((2, 3 * chips)),
            dma((2, 3 * chips + 1)),
            dma((2, 3 * chips)),
            dma((2, 3 * chips + 1)),
            dma((2, members)),
            dma((8,)),
            dma((2,)),
        ],
        compiler_params=pltpu.CompilerParams(
            collective_id=0, has_side_effects=True, vmem_limit_bytes=60 * 1024 * 1024
        ),
        name="forward",
    )(lengths, bias_table, routes_t, tokens, cotangent, gains, router, attn_qkv, attn_out, expert_in, expert_out)


def expert_kernel(
    grps,
    exps,
    cap,
    deal,
    routes_t,
    comb,
    n_all,
    cot_all,
    both_w,
    down_w,
    in_low,
    down_slab,
    h1,
    n_total,
    y_half,
    y_far,
    c_in,
    both_g,
    down_g,
    in_parts,
    down_parts,
    place,
    marks,
    n_rows,
    g_rows,
    both_v,
    down_v,
    raw_n,
    raw_g,
    y_acc,
    n_acc,
    both_d,
    active,
    n_bufs,
    c_sum,
    out_y,
    load_sem,
    raw_sem,
    out_sem,
    in_sem,
    in_down_sem,
    home_sem,
    home_down_sem,
    stage_sem,
    far_sem,
    n_sem,
    c_sem,
):
    at = Where(grps, exps)
    rows, width = n_all.shape[1:]
    tiles = Tiles(down_slab.shape[0], at.reps)
    size = tiles.size
    slots = exps * cap
    members = QUAD * exps
    loads = [pltpu.make_async_copy(both_w.at[t], both_v.at[t], load_sem.at[0, t]) for t in range(2)] + [
        pltpu.make_async_copy(down_w.at[t], down_v.at[t], load_sem.at[1, t]) for t in range(2)
    ]
    for copy in loads:
        copy.start()

    def raw_copies(q):
        here = pl.ds(pl.multiple_of(q * exps, exps), exps)
        return [
            pltpu.make_async_copy(n_all.at[here], raw_n.at[pl.ds(q % 2 * exps, exps)], raw_sem.at[0, q % 2]),
            pltpu.make_async_copy(cot_all.at[here], raw_g.at[pl.ds(q % 2 * exps, exps)], raw_sem.at[1, q % 2]),
        ]

    for copy in raw_copies(0):
        copy.start()

    beside = at.exp + 1 - 2 * (at.exp % 2)
    greet(*neighbours(at))()
    last = tiles.count - 1
    incoming = Outward(
        at, tiles, last, in_low, down_slab, both_v.at[last], down_v.at[last], None, in_sem, in_down_sem
    )
    incoming.start()
    home = Homeward(
        at, tiles, 0, both_v.at[0], down_v.at[0], in_parts, down_parts, home_sem, home_down_sem, (0,)
    )

    earlier = jnp.where(row_of((rows, rows)) < lane_of((rows, rows)), 1.0, 0.0).astype(low)
    slot = row_of((cap, rows)).astype(full)

    def dispatch(q, _):
        @pl.when(q + 1 < QUAD)
        def _():
            for copy in raw_copies(q + 1):
                copy.start()

        for copy in raw_copies(q):
            copy.wait()
        lines = []
        for j in range(exps):
            seq = at.grp * members + q * exps + j
            pair = routes_t[:, pl.ds(pl.multiple_of(seq * rows, rows), rows)]
            lines.append(jnp.logical_or(pair[0:1] == at.exp, pair[1:2] == at.exp))
        lines = [jnp.where(line, 1.0, 0.0) for line in lines] + [jnp.zeros((8 - exps, rows), full)]
        hot_low = jnp.concatenate(lines, axis=0).astype(low)
        before = dot(hot_low, earlier)
        for j in range(exps):
            s = q * exps + j
            inside = jnp.logical_and(slot == before[j : j + 1, :], hot_low[j : j + 1, :].astype(full) > 0.5)
            here = jnp.where(inside, 1.0, 0.0)
            place[s] = here.astype(low)
            g = raw_g[q % 2 * exps]
            for b in range(1, exps):
                g = jnp.where(deal[at.grp * members + s] == at.grp * members + q * exps + b, raw_g[q % 2 * exps + b], g)
            where = pl.ds(pl.multiple_of(s * cap, cap), cap)
            n_rows[where] = dot(here.astype(low), raw_n[q % 2 * exps + j]).astype(low)
            g_rows[where] = dot(here.astype(low), g).astype(low)
            marks[where, 0:1] = jnp.sum(here * comb[s, pl.ds(at.exp, 1), :], axis=1, keepdims=True)
            marks[where, 1:2] = jnp.zeros((cap, 1), full)
        return 0

    lax.fori_loop(0, QUAD, dispatch, 0)
    for copy in loads:
        copy.wait()
    curve = math.sqrt(2.0 / math.pi)

    core = at.exp % 2

    plane = at.quad * exps + at.exp
    sibling = at.device(at.rep, beside)
    dn = Halving(at, n_bufs, n_sem, [[0, 1, 2], [1, 2, 0], [2, 0, 1]])

    def n_copy(j):
        return send(raw_n.at[j], n_bufs[0].at[j], far_sem.at[0, 0, j], far_sem.at[0, 1, j], sibling)

    def y_copies(j):
        return (
            pltpu.make_async_copy(out_y.at[j % 2], y_half.at[j], out_sem.at[j % 2]),
            send(raw_n.at[j], y_far.at[j], far_sem.at[1, 0, j], far_sem.at[1, 1, j], sibling),
        )

    def c_copy(k):
        other = (plane + k) % members
        return send(
            c_sum.at[other],
            c_in.at[plane],
            c_sem.at[0, other],
            c_sem.at[1, plane],
            (at.grp, other // exps, other % exps),
        )

    def slots_of(s):
        return pl.ds(pl.multiple_of(s * cap, cap), cap)

    def n_rows_of(s):
        where = slots_of(s)
        line = jnp.sum(place[s].astype(full) * marks[where, 1:2], axis=0, keepdims=True)
        c_sum[s] = jnp.broadcast_to(line, (8, rows))
        return tn(place[s], n_acc[where]).astype(low)

    def y_rows_of(p):
        first = p // exps * exps
        spot = at.grp * members + p
        here, y = place[first], y_acc[slots_of(first)]
        for c in range(1, exps):
            taken = deal[at.grp * members + first + c] == spot
            here = jnp.where(taken, place[first + c], here)
            y = jnp.where(taken, y_acc[slots_of(first + c)], y)
        return (tn(here, y) + jnp.where(deal[at.me] == spot, h1[...], 0.0)).astype(low)

    def give_n(j, _):
        raw_n[j] = n_rows_of(2 * j + 1 - core)
        n_copy(j).start()
        raw_g[j] = n_rows_of(2 * j + core)
        return 0

    def add_n(j, _):
        arrived(n_bufs[0].at[j], far_sem.at[0, 1, j])
        n_bufs[0][j] = n_bufs[0][j] + raw_g[j]
        return 0

    def give_y(j, _):
        @pl.when(j >= 2)
        def _():
            y_copies(j - 2)[0].wait()

        out_y[j % 2] = y_rows_of(2 * j + core)
        n_copy(j).wait_send()
        raw_n[j] = y_rows_of(2 * j + 1 - core)
        for copy in y_copies(j):
            copy.start()
        return 0

    def start_c(k, _):
        c_copy(k).start()
        return 0

    def tile_work(f, _):
        @pl.when(f == last)
        def _():
            incoming.arrive()

        def chunk(c, _):
            here = pl.ds(pl.multiple_of(c * slots, slots), slots)
            share = marks[here, 0:1]
            both = dot(n_rows[here], both_v[f])
            gate_part, up_part = both[:, :size], both[:, size:]
            grad = nt(g_rows[here], down_v[f])
            square = gate_part * gate_part
            bend = jnp.tanh(curve * gate_part * (1.0 + 0.044715 * square))
            half = 0.5 * (1.0 + bend)
            gelu = gate_part * half
            slope = half + (0.5 * curve) * gate_part * (1.0 - bend * bend) * (1.0 + (3 * 0.044715) * square)
            value = gelu * up_part
            marks[here, 1:2] += jnp.sum(value * grad, axis=1, keepdims=True)
            grad = grad * share
            active[f, here] = (value * share).astype(low)
            both_d[f, here, :size] = (grad * up_part * slope).astype(low)
            both_d[f, here, size:] = (grad * gelu).astype(low)
            y = dot(active[f, here], down_v[f])
            y_acc[here] = jnp.where(f == 0, y, y_acc[here].astype(full) + y).astype(low)
            n_back = nt(both_d[f, here], both_v[f])
            n_acc[here] = jnp.where(f == 0, n_back, n_acc[here].astype(full) + n_back).astype(low)
            return 0

        lax.fori_loop(0, QUAD, chunk, 0)

        @pl.when(f == 0)
        def _():
            weight_work(0)

        return 0

    def weight_work(f):
        def columns(m, _):
            cols = pl.ds(pl.multiple_of(m * (width // 2), width // 2), width // 2)
            both_v[f, cols] = tn(n_rows[:, cols], both_d[f]).astype(low)
            down_v[f, :, cols] = tn(active[f], g_rows[:, cols]).astype(low)
            return 0

        lax.fori_loop(0, 2, columns, 0)

        for copy in stage_copies(f):
            copy.start()
        if f == 0:
            home.start()

    def stage_copies(f):
        copies = [pltpu.make_async_copy(both_v.at[f], both_g.at[f], stage_sem.at[0, f])]
        if f:
            copies.append(pltpu.make_async_copy(down_v.at[f], down_g.at[f - 1], stage_sem.at[1, f]))
        return copies

    lax.fori_loop(0, tiles.count, tile_work, 0)

    half = members // 2
    lax.fori_loop(0, half, give_n, 0)
    lax.fori_loop(1, members, start_c, 0)
    c_in[plane] = c_sum[plane]
    weight_work(1)
    lax.fori_loop(0, half, add_n, 0)
    dn.start(0)
    weight_work(2)
    lax.fori_loop(0, half, give_y, 0)
    for step in range(len(dn.chip_bits)):
        dn.next(step)
    n_total[...] = dn.result()[0]
    for j in (half - 2, half - 1):
        y_copies(j)[0].wait()
    for f in range(tiles.count):
        for copy in stage_copies(f):
            copy.wait()

    def core_in(j, _):
        y_copies(j)[1].wait_send()
        arrived(y_far.at[j], far_sem.at[1, 1, j])
        return 0

    lax.fori_loop(0, half, core_in, 0)

    def c_done(k, _):
        c_copy(k).wait_send()
        other = (plane + k) % members
        arrived(c_in.at[other], c_sem.at[1, other])
        return 0

    lax.fori_loop(1, members, c_done, 0)
    dn.finish()
    home.arrive()
    incoming.sent()
    home.sent()


def expert_call(grps, exps, cap, deal, routes_t, comb_all, n_all, cot_all, both_w, down_w, in_low, down_slab, h1):
    members, rows, width = n_all.shape
    reps = grps * QUAD
    tiles = Tiles(down_slab.shape[0], reps)
    size = tiles.size
    slab, both_hidden = in_low.shape
    units = down_slab.shape[0]
    slots = exps * cap
    chip_bits = bits_of(members) - 1
    shape = jax.ShapeDtypeStruct
    vmem = pl.BlockSpec(memory_space=pltpu.VMEM)
    smem = pl.BlockSpec(memory_space=pltpu.SMEM)
    hbm = pl.BlockSpec(memory_space=pl.ANY)
    results = [
        (shape((rows, width), low), vmem),
        (shape((members // 2, rows, width), low), hbm),
        (shape((members // 2, rows, width), low), hbm),
        (shape((members, 8, rows), full), vmem),
        (shape((tiles.count, width, 2 * size), low), hbm),
        (shape((2, size, width), low), hbm),
        (shape((grps, slab, both_hidden), low), hbm),
        (shape((grps, units, width), low), hbm),
    ]
    dma = pltpu.SemaphoreType.DMA
    return pl.pallas_call(
        functools.partial(expert_kernel, grps, exps, cap),
        out_shape=[r[0] for r in results],
        in_specs=[smem] + [vmem] * 2 + [hbm] * 6 + [vmem],
        out_specs=[r[1] for r in results],
        scratch_shapes=[
            pltpu.VMEM((members, cap, rows), low),
            pltpu.VMEM((QUAD * slots, 128), full),
            pltpu.VMEM((QUAD * slots, width), low),
            pltpu.VMEM((QUAD * slots, width), low),
            pltpu.VMEM((tiles.count, width, 2 * size), low),
            pltpu.VMEM((tiles.count, size, width), low),
            pltpu.VMEM((2 * exps, rows, width), low),
            pltpu.VMEM((2 * exps, rows, width), low),
            pltpu.VMEM((QUAD * slots, width), low),
            pltpu.VMEM((QUAD * slots, width), low),
            pltpu.VMEM((tiles.count, QUAD * slots, 2 * size), low),
            pltpu.VMEM((tiles.count, QUAD * slots, size), low),
            [pltpu.VMEM((members >> (1 + step), rows, width), low) for step in range(chip_bits + 1)],
            pltpu.VMEM((members, 8, rows), full),
            pltpu.VMEM((2, rows, width), low),
            dma((2, 2)),
            dma((2, 2)),
            dma((2,)),
            dma((2, 2 * reps)),
            dma((2, reps + 1)),
            dma((2, 2 * reps)),
            dma((2, max(QUAD, grps))),
            dma((2, tiles.count)),
            dma((2, 2, members // 2)),
            dma((2, 3 << chip_bits)),
            dma((2, members)),
        ],
        compiler_params=pltpu.CompilerParams(
            collective_id=2, has_side_effects=True, vmem_limit_bytes=60 * 1024 * 1024
        ),
        name="experts",
    )(deal, routes_t, comb_all, n_all, cot_all, both_w, down_w, in_low, down_slab, h1)


def adamw_root(weight, moment, second, gradient, step_rate, decay_factor):
    new_moment = beta_one * moment + (1.0 - beta_one) * gradient
    new_second = beta_two * second + (1.0 - beta_two) * gradient * gradient
    root = lax.rsqrt(new_second * (1.0 / (1.0 - beta_two**STEP)))
    step = new_moment * (root * (1.0 - eps_adam * root))
    keep = 1.0 - step_rate * decay_factor
    return (new_moment, new_second, keep * weight - (step_rate / (1.0 - beta_one**STEP)) * step)


def adam_kernel(exps, *refs):
    in_parts, down_parts, qkv_grad, out_grad, small = refs[:5]
    states, news, bias_grad = refs[5:26], refs[26:47], refs[47]
    heads = HEADS // exps
    width = small.shape[1]

    def update(i, grad, rate, decay):
        weight, first, second = [state[...] for state in states[3 * i : 3 * i + 3]]
        values = adamw_root(weight, first, second, grad, rate, decay)
        for new, value in zip(news[3 * i : 3 * i + 3], values, strict=True):
            new[...] = value

    def total(parts):
        result = parts[0].astype(full)
        for k in range(1, parts.shape[0]):
            result = result + parts[k].astype(full)
        return result

    @pl.when(pl.program_id(0) == 0)
    def _():
        update(0, qkv_grad[...], 1.5 / math.sqrt(D), 0.1)
        update(1, out_grad[...], 6.0 / math.sqrt(D), 0.1)
        for e in range(exps):
            for h in range(heads):
                bias_grad[e * heads + h : e * heads + h + 1, :] = small[
                    exps + 3 + e : exps + 4 + e, h * 128 : h * 128 + BUCKETS
                ]
        update(2, bias_grad[...], 0.3, 0.0)
        update(3, small[0:exps, :], 1.0 / math.sqrt(D), 0.1)
        update(4, small[exps : exps + 2, :], 0.5, 0.0)

    update(5, total(in_parts), 1.5 / math.sqrt(D), 0.1)
    update(6, total(down_parts), 1.5 / math.sqrt(FF), 0.1)


def adam_call(exps, in_parts, down_parts, qkv_grad, out_grad, small, states):
    steps = 4

    def whole(array):
        return pl.BlockSpec(array.shape, lambda i: (0,) * array.ndim)

    def columns(array):
        block = array.shape[:-1] + (array.shape[-1] // steps,)
        return pl.BlockSpec(block, lambda i: (0,) * (array.ndim - 1) + (i,))

    specs = [whole(state) for state in states[:15]]
    specs += [columns(state) for state in states[15:18]] + [columns(state) for state in states[18:]]
    return pl.pallas_call(
        functools.partial(adam_kernel, exps),
        grid=(steps,),
        in_specs=[columns(in_parts), columns(down_parts), whole(qkv_grad), whole(out_grad), whole(small)] + specs,
        out_specs=specs,
        out_shape=[jax.ShapeDtypeStruct(state.shape, full) for state in states],
        scratch_shapes=[pltpu.VMEM((HEADS, BUCKETS), full)],
        compiler_params=pltpu.CompilerParams(vmem_limit_bytes=60 * 1024 * 1024),
        name="adam",
    )(in_parts, down_parts, qkv_grad, out_grad, small, *states)


def backward_kernel(
    grps,
    exps,
    lengths,
    deal,
    bias_table,
    y_half,
    y_far,
    both_g,
    down_g,
    in_before,
    down_before,
    n1_in,
    cot_all,
    routes_t,
    tokens,
    n_total,
    c_in,
    n2_in,
    probs_in,
    h1_from,
    qkv_from,
    lse_from,
    mine_from,
    wqkv_from,
    wout_from,
    gains,
    router_t,
    *rest,
):
    token_grad, block_out, in_parts, down_parts, qkv_grad, out_grad, small_out = rest[:7]
    scratch = rest[7:]
    (
    h1_in,
    qkv,
    lse,
    mine,
    wqkv,
    wout,
    kept,
    y_bufs,
    dh1,
    dz_send,
    dz_all,
    do_send,
    do_in,
    bias,
    bias_sum,
    dqkv,
    dqkv_t,
    dn1_send,
    dn1_in,
    wq_send,
    og_send,
    mids,
    far_send,
    far_in,
    small_send,
    small_exp,
    small_sum,
    small_rep,
    y_sem,
    load_sem,
    weight_sem,
    down_sem,
    dz_sem,
    do_sem,
    dn1_sem,
    wq_sem,
    og_sem,
    mid_sem,
    far_sem,
    small_sem,
    small2_sem,
    n1_sem,
    operand_sem,
    ) = scratch
    at = Where(grps, exps)
    reps = at.reps
    rows, width = tokens.shape
    heads = HEADS // exps
    head_dim = width // HEADS
    head_cols = heads * head_dim
    block_cols = min(128, head_cols)
    row_block = wqkv.shape[2]
    out_cols = wout.shape[3]
    tiles = Tiles(down_parts.shape[1], reps)
    scale = 1.0 / math.sqrt(head_dim)
    SEND, RECV = 0, 1
    plane = at.quad * exps + at.exp
    members = QUAD * exps

    def exp_peer(k):
        return (at.exp + k) % exps

    router = router_t[...]
    met = greet(*neighbours(at))
    n1 = kept.at[0:exps]
    group = pl.ds(pl.multiple_of(at.quad * exps, exps), exps)
    cot_copy = pltpu.make_async_copy(cot_all.at[group], dn1_send, n1_sem.at[1])
    cot_copy.start()
    loads = [
        pltpu.make_async_copy(src, dst, operand_sem.at[i])
        for i, (src, dst) in enumerate(
            ((h1_from, h1_in), (wout_from, wout), (qkv_from, qkv), (lse_from, lse), (mine_from, mine), (wqkv_from, wqkv))
        )
    ]
    ys = Halving(at, y_bufs, y_sem, [[0, 1, 2], [0, 1, 2], [1, 0, 2]])
    half_loads = [
        pltpu.make_async_copy(y_far, y_bufs[0], load_sem.at[0]),
        pltpu.make_async_copy(y_half, kept, load_sem.at[1]),
    ]
    for copy in loads + half_loads:
        copy.start()

    span = 2 * rows
    bucket = bucket_of(lane_of((8, span)) - rows)
    for h in range(heads):
        line = jnp.zeros((8, span), full)
        for b in range(BUCKETS):
            line = jnp.where(bucket == b, bias_table[at.exp * heads + h, b], line)
        whole = jnp.broadcast_to(line[0:1], (rows, span))
        bias[h] = pltpu.roll(whole, 0, 1, stride=1, stride_axis=0)[:, rows:]


    met()

    homes = [
        Homeward(
            at,
            tiles,
            t,
            both_g.at[t],
            down_g.at[t - 1] if t else None,
            in_parts,
            down_parts,
            weight_sem.at[t],
            down_sem.at[t],
            (0, 1) if t else (1,),
        )
        for t in range(tiles.count)
    ]
    homes[0].start()
    homes[1].start()
    n1_copy = pltpu.make_async_copy(n1_in, n1, n1_sem.at[0])

    lane = lane_of((rows, 128))
    comb_rows = []
    for e in range(exps):
        total = c_in[e]
        for q in range(1, QUAD):
            total = total + c_in[q * exps + e]
        comb_rows.append(total[0:1, :])
    comb_rows.append(jnp.zeros((128 - exps, rows), full))
    comb_grad = jnp.concatenate(comb_rows, axis=0).T
    valid = row_of((rows, 1)) < lengths[at.me]
    probs = probs_in[...]
    hot = routed(routes_t, at.me, rows)
    picked = jnp.where(hot, probs, 0.0)
    total = jnp.sum(picked, axis=1, keepdims=True)
    gate = picked / total
    gate_grad_rows = jnp.where(valid, comb_grad, 0.0)
    spread_grad = jnp.sum(gate_grad_rows * gate, axis=1, keepdims=True)
    probs_grad = jnp.where(hot, (gate_grad_rows - spread_grad) / total, 0.0)
    logit_grad = probs * (probs_grad - jnp.sum(probs_grad * probs, axis=1, keepdims=True))
    small_rows = small_send.shape[0]
    small_send[...] = jnp.zeros_like(small_send)
    router_back = jnp.dot(
        logit_grad, jnp.concatenate([router, jnp.zeros((128 - exps, width), full)], axis=0),
        precision=highest, preferred_element_type=full,
    )
    for copy in loads:
        copy.wait()
    h1 = h1_in[...]
    r2 = lax.rsqrt(jnp.mean(h1 * h1, axis=1, keepdims=True) + eps_norm)

    steps = len(ys.chip_bits)
    n2_grad = router_back + n_total[...].astype(full)
    scaled = n2_grad * gains[1:2, :]
    cot_copy.wait()
    dealt = deal[at.me] - at.base
    g = dn1_send[0]
    for e in range(1, exps):
        g = jnp.where(dealt == e, dn1_send[e], g)
    hidden_grad = (
        jnp.where(valid, g.astype(full), 0.0)
        + r2 * scaled
        - h1 * (r2 * r2 * r2) * jnp.mean(scaled * h1, axis=1, keepdims=True)
    )
    dh1[...] = hidden_grad
    small_send[exps + 1 : exps + 2, :] = jnp.sum(n2_grad * h1 * r2, axis=0, keepdims=True)
    branch = hidden_grad.astype(low)
    dz_send[...] = branch
    for e in range(exps):
        total = jnp.zeros((rows, row_block), full)
        for r in range(reps):
            total = total + nt(branch[:, r * out_cols : (r + 1) * out_cols], wout[e, r])
        do_send[e] = total.astype(low)

    def do_copies():
        return [
            send(
                do_send.at[exp_peer(k)],
                do_in.at[at.exp],
                do_sem.at[SEND, exp_peer(k)],
                do_sem.at[RECV, at.exp],
                at.device(at.rep, exp_peer(k)),
            )
            for k in range(1, exps)
        ]

    for copy in do_copies():
        copy.start()
    pltpu.make_async_copy(do_send.at[at.exp], do_in.at[at.exp], do_sem.at[RECV, at.exp]).start()

    group_dz = Group(at, dz_send, dz_all, dz_sem)
    group_dz.start()
    dz_all[at.exp] = branch
    for copy in half_loads:
        copy.wait()

    def add_halves(j, _):
        y_bufs[0][j] = y_bufs[0][j] + kept[j]
        return 0

    lax.fori_loop(0, kept.shape[0], add_halves, 0)
    ys.start(0)
    n1_copy.start()

    bias_sum[...] = jnp.zeros_like(bias_sum)

    def dn1_copies():
        beside, across = turn(at.exp, 2), turn(at.exp, 1)
        return [
            functools.partial(
                send, dn1_send.at[k], dn1_in.at[j], dn1_sem.at[SEND, j], dn1_sem.at[RECV, j], at.device(at.rep, to)
            )
            for k, j, to in ((turn(at.exp, 0), 2, beside), (across, 0, across), (beside, 1, beside))
        ]

    def attend_back(i, _):
        s = turn(at.exp, i)
        @pl.when(i == 1)
        def _():
            group_dz.pass_on()

        arrived(do_in.at[s], do_sem.at[RECV, s])
        ok = lane_of((rows, rows)) < lengths[at.base + s]
        block_lane = lane_of((rows, block_cols))
        for c in range(head_cols // block_cols):
            cols = slice(c * block_cols, (c + 1) * block_cols)
            k_cols = slice(head_cols + c * block_cols, head_cols + (c + 1) * block_cols)
            v_cols = slice(2 * head_cols + c * block_cols, 2 * head_cols + (c + 1) * block_cols)
            q = qkv[s, :, cols] * scale
            k = qkv[s, :, k_cols]
            v = qkv[s, :, v_cols]
            do = do_in[s, :, cols]
            dq = jnp.zeros((rows, block_cols), full)
            dk = jnp.zeros((rows, block_cols), full)
            dv = jnp.zeros((rows, block_cols), full)
            for t in range(block_cols // head_dim):
                h = c * (block_cols // head_dim) + t
                here = jnp.logical_and(block_lane >= t * head_dim, block_lane < (t + 1) * head_dim)
                zero = jnp.zeros_like(q)
                q_h = jnp.where(here, q, zero)
                do_h = jnp.where(here, do, zero)
                scores = nt(q_h, k) + bias[h]
                p = jnp.where(ok, jnp.exp(scores - lse[s, :, h : h + 1]), 0.0)
                dp = nt(do_h, v)
                delta = jnp.sum(dp * p, axis=1, keepdims=True)
                ds = (p * (dp - delta)).astype(low)
                bias_sum[h] += ds.astype(full)
                dv = jnp.where(here, tn(p.astype(low), do), dv)
                dq = jnp.where(here, jnp.dot(ds, k, preferred_element_type=full), dq)
                dk = jnp.where(here, tn(ds, q), dk)
            dqkv[:, cols] = (dq * scale).astype(low)
            dqkv[:, k_cols] = dk.astype(low)
            dqkv[:, v_cols] = dv.astype(low)
        dqkv_t[:, pl.ds(pl.multiple_of(s * rows, rows), rows)] = dqkv[...].T
        for e in range(exps):
            dn1_send[s, :, e * row_block : (e + 1) * row_block] = jnp.dot(
                dqkv[...], wqkv[e], preferred_element_type=full
            ).astype(low)

        @pl.when(i == 0)
        def _():
            dn1_copies()[0]().start()

        @pl.when(i == 1)
        def _():
            arrived(dn1_in.at[2], dn1_sem.at[RECV, 2])
            dn1_send[s] = (dn1_send[s].astype(full) + dn1_in[2].astype(full)).astype(low)
            dn1_copies()[1]().start()

        @pl.when(i == 2)
        def _():
            dn1_copies()[2]().start()

        return 0

    lax.fori_loop(0, exps, attend_back, 0)

    n1_copy.wait()
    seg = wq_send.shape[2]
    parts = wq_send.shape[1]
    segs = mids.shape[1] - 1
    for e in range(exps):
        part = kept[0:exps, :, e * row_block : (e + 1) * row_block].reshape(exps * rows, row_block)
        total = dot(dqkv_t[...], part)
        for j in range(parts):
            wq_send[e, j] = total[j * seg : (j + 1) * seg].astype(low)

    def owner(j):
        section, within = j // (head_cols // seg), j % (head_cols // seg)
        col = section * width + at.exp * head_cols + within * seg
        block = col // seg
        return block // segs, block % segs

    def mid_place(grp, k, quad):
        return (grp * (segs + 1) + k) * QUAD + quad

    def mid_copy(src, send_sem, rep, k, e):
        dst = mids.at[rep // QUAD, k, at.quad]
        recv = mid_sem.at[mid_place(rep // QUAD, k, at.quad)]
        stays = jnp.logical_and(rep % QUAD == at.quad, e == at.exp)
        return (
            stays,
            functools.partial(send, src, dst, send_sem, recv, (at.grp, rep % QUAD, e)),
            functools.partial(pltpu.make_async_copy, src, dst, recv),
        )

    def wq_copy(i):
        e, j = i // parts, i % parts
        rep, k = owner(j)
        return mid_copy(wq_send.at[e, j], wq_sem.at[i], rep, k, e)

    def og_copy(r):
        return mid_copy(og_send.at[r], og_sem.at[r], r, segs, at.exp)

    def go(copies, act, act_local):
        stays, away, local = copies

        @pl.when(jnp.logical_not(stays))
        def _():
            act(away)

        if act_local:

            @pl.when(stays)
            def _():
                act_local(local)

    def over(count, copies, act, act_local):
        def one(i, _):
            go(copies(i), act, act_local)
            return 0

        lax.fori_loop(0, count, one, 0)

    over(exps * parts, wq_copy, lambda copy: copy().start(), lambda copy: copy().start())
    group_dz.arrive()
    grad = tn(mine[...].reshape(exps * rows, head_cols), dz_all[...].reshape(exps * rows, width))
    for r in range(reps):
        og_send[r] = grad[:, r * out_cols : (r + 1) * out_cols].T.astype(low)
    over(reps, og_copy, lambda copy: copy().start(), lambda copy: copy().start())
    homes[2].start()

    n1_grad = dn1_send[at.exp].astype(full)
    for j in range(2):
        arrived(dn1_in.at[j], dn1_sem.at[RECV, j])
        n1_grad = n1_grad + dn1_in[j].astype(full)
    x = tokens[...].astype(full)
    r1 = lax.rsqrt(jnp.mean(x * x, axis=1, keepdims=True) + eps_norm)
    scaled = n1_grad * gains[0:1, :]
    token_grad[...] = (
        dh1[...] + r1 * scaled - x * (r1 * r1 * r1) * jnp.mean(scaled * x, axis=1, keepdims=True)
    )
    small_send[exps : exps + 1, :] = jnp.sum(n1_grad * x * r1, axis=0, keepdims=True)

    router_rows = lax.dot_general(
        logit_grad, n2_in[...].astype(full), (((0,), (0,)), ((), ())), preferred_element_type=full, precision=highest
    )
    small_send[0:exps, :] = router_rows[0:exps, :]

    line_lane = lane_of((8, 128))
    line_row = row_of((8, 128))
    bias_line = jnp.zeros((8, 128), full)
    flip = jnp.where(row_of((rows, rows)) + lane_of((rows, rows)) == rows - 1, 1.0, 0.0).astype(low)
    turned_bucket = bucket_of(rows - 1 - lane_of((8, span)))
    for h in range(heads):
        high = bias_sum[h].astype(low)
        rest = (bias_sum[h] - high.astype(full)).astype(low)
        flipped = dot(high, flip) + dot(rest, flip)
        square = jnp.concatenate([flipped, jnp.zeros((rows, rows), full)], axis=1)
        turned = pltpu.roll(square, 0, 1, stride=1, stride_axis=0)
        sums = jnp.broadcast_to(jnp.sum(turned, axis=0, keepdims=True), (8, span))
        for b in range(BUCKETS):
            value = jnp.sum(jnp.where(turned_bucket == b, sums, 0.0), axis=1, keepdims=True)
            bias_line = jnp.where(jnp.logical_and(line_row == h, line_lane == b), value, bias_line)
    for h in range(heads):
        small_send[exps + 2 : exps + 3, h * 128 : (h + 1) * 128] = bias_line[h : h + 1, :]

    def small_copies():
        return [
            send(
                small_send,
                small_exp.at[at.exp],
                small_sem.at[SEND, exp_peer(k)],
                small_sem.at[RECV, at.exp],
                at.device(at.rep, exp_peer(k)),
            )
            for k in range(1, exps)
        ]

    for copy in small_copies():
        copy.start()
    small_exp[at.exp] = small_send[...]
    ys.next(0)

    def mid_sum(grp, k):
        for q in range(QUAD):
            arrived(mids.at[grp, k, q], mid_sem.at[mid_place(grp, k, q)])
        total = mids[grp, k, 0].astype(full)
        for q in range(1, QUAD):
            total = total + mids[grp, k, q].astype(full)
        return total

    far = 1 - at.grp
    for k in range(segs + 1):
        far_send[k] = mid_sum(far, k).astype(low)

    def far_copy():
        return send(far_send, far_in, far_sem.at[SEND], far_sem.at[RECV], (far, at.quad, at.exp))

    far_copy().start()
    ys.next(1)
    for k in range(1, exps):
        arrived(small_exp.at[exp_peer(k)], small_sem.at[RECV, exp_peer(k)])
    total = small_exp[0]
    for e in range(1, exps):
        total = total + small_exp[e]
    small_sum[0] = total
    for e in range(exps):
        small_sum[0, exps + 3 + e : exps + 4 + e, :] = small_exp[e, exps + 2 : exps + 3, :]

    def small2_copies():
        return [
            send(
                small_sum.at[0],
                small_rep.at[at.rep],
                small2_sem.at[SEND, (at.rep + k) % reps],
                small2_sem.at[RECV, at.rep],
                at.device((at.rep + k) % reps, at.exp),
            )
            for k in range(1, reps)
        ]

    for copy in small2_copies():
        copy.start()
    small_rep[at.rep] = small_sum[0]
    for step in range(2, steps):
        ys.next(step)
    length = lengths[at.base]
    for e in range(1, exps):
        length = jnp.where(deal[at.base + e] == at.me, lengths[at.base + e], length)
    block = ys.result()[0]
    block_out[...] = jnp.where(row_of((rows, 1)) < length, block, jnp.zeros_like(block))
    for k in range(1, reps):
        arrived(small_rep.at[(at.rep + k) % reps], small2_sem.at[RECV, (at.rep + k) % reps])
    total = small_rep[0]
    for r in range(1, reps):
        total = total + small_rep[r]
    small_out[...] = total

    near = [mid_sum(at.grp, k) for k in range(segs + 1)]
    arrived(far_in, far_sem.at[RECV])
    grads = [(near[k] + far_in[k].astype(full)).T for k in range(segs + 1)]
    qkv_grad[...] = jnp.concatenate(grads[:segs], axis=1)
    out_grad[...] = grads[segs]
    for home in homes:
        home.arrive()

    ys.finish()

    for home in homes:
        home.sent()

    over(exps * parts, wq_copy, lambda copy: copy().wait_send(), None)
    over(reps, og_copy, lambda copy: copy().wait_send(), None)
    far_copy().wait_send()
    for copies in (do_copies(), small_copies(), small2_copies()):
        for copy in copies:
            copy.wait_send()
    for copy in dn1_copies():
        copy().wait_send()
    group_dz.sent()


def routed(routes_t, seq, rows):
    pair = routes_t[:, pl.ds(pl.multiple_of(seq * rows, rows), rows)].astype(full)
    cols = jnp.concatenate([pair, jnp.zeros((126, rows), full)], axis=0).T
    lane = lane_of((rows, 128)).astype(full)
    return jnp.logical_or(lane == cols[:, 0:1], lane == cols[:, 1:2])


def backward_call(
    grps, exps, lengths, deal, bias_table, y_half, y_far, both_g, down_g, in_before, down_before, n1,
    cot_all, routes_t, tokens, n_total, c_in, n2, probs, h1, qkv, lse, mine, wqkv, wout, gains, router
):
    reps = grps * QUAD
    rows, width = tokens.shape
    heads = HEADS // exps
    head_cols = width // exps
    row_block = wqkv.shape[2]
    out_cols = wout.shape[3]
    shard_cols = 3 * width // reps
    seg = math.gcd(shard_cols, head_cols)
    segs = shard_cols // seg
    parts = 3 * head_cols // seg
    members = QUAD * exps
    chip_bits = bits_of(members) - 1
    small_rows = -(-(2 * exps + 3) // 8) * 8
    shape = jax.ShapeDtypeStruct
    vmem = pl.BlockSpec(memory_space=pltpu.VMEM)
    smem = pl.BlockSpec(memory_space=pltpu.SMEM)
    hbm = pl.BlockSpec(memory_space=pl.ANY)
    results = [
        (shape((rows, width), full), vmem),
        (shape((rows, width), low), vmem),
        (shape(in_before.shape, low), hbm),
        (shape(down_before.shape, low), hbm),
        (shape((row_block, shard_cols), full), vmem),
        (shape((row_block, out_cols), full), vmem),
        (shape((small_rows, width), full), vmem),
    ]
    dma = pltpu.SemaphoreType.DMA
    bufs = [pltpu.VMEM((1 << (chip_bits - s), rows, width), low) for s in range(chip_bits + 1)]
    return pl.pallas_call(
        functools.partial(backward_kernel, grps, exps),
        out_shape=[r[0] for r in results],
        in_specs=[smem] * 3 + [hbm] * 8 + [vmem] * 6 + [hbm] * 6 + [vmem] * 2,
        out_specs=[r[1] for r in results],
        scratch_shapes=[
            pltpu.VMEM(h1.shape, full),
            pltpu.VMEM(qkv.shape, low),
            pltpu.VMEM(lse.shape, full),
            pltpu.VMEM(mine.shape, low),
            pltpu.VMEM(wqkv.shape, low),
            pltpu.VMEM(wout.shape, low),
            pltpu.VMEM((members // 2, rows, width), low),
            list(bufs),
            pltpu.VMEM((rows, width), full),
            pltpu.VMEM((rows, width), low),
            pltpu.VMEM((exps, rows, width), low),
            pltpu.VMEM((exps, rows, head_cols), low),
            pltpu.VMEM((exps, rows, head_cols), low),
            pltpu.VMEM((heads, rows, rows), full),
            pltpu.VMEM((heads, rows, rows), full),
            pltpu.VMEM((rows, 3 * head_cols), low),
            pltpu.VMEM((3 * head_cols, exps * rows), low),
            pltpu.VMEM((exps, rows, width), low),
            pltpu.VMEM((3, rows, width), low),
            pltpu.VMEM((exps, parts, seg, row_block), low),
            pltpu.VMEM((reps, seg, row_block), low),
            pltpu.VMEM((grps, segs + 1, QUAD, seg, row_block), low),
            pltpu.VMEM((segs + 1, seg, row_block), low),
            pltpu.VMEM((segs + 1, seg, row_block), low),
            pltpu.VMEM((small_rows, width), full),
            pltpu.VMEM((exps, small_rows, width), full),
            pltpu.VMEM((1, small_rows, width), full),
            pltpu.VMEM((reps, small_rows, width), full),
            dma((2, 3 << chip_bits)),
            dma((2,)),
            dma((3, 2, 2 * reps)),
            dma((3, 2, max(QUAD, grps))),
            dma((2, exps)),
            dma((2, exps)),
            dma((2, exps)),
            dma((exps * parts,)),
            dma((reps,)),
            dma((grps * (segs + 1) * QUAD,)),
            dma((2,)),
            dma((2, exps)),
            dma((2, reps)),
            dma((2,)),
            dma((6,)),
        ],
        compiler_params=pltpu.CompilerParams(
            collective_id=1, has_side_effects=True, vmem_limit_bytes=60 * 1024 * 1024
        ),
        input_output_aliases={7: 2, 8: 3},
        name="backward",
    )(
        lengths, deal, bias_table, y_half, y_far, both_g, down_g, in_before, down_before, n1, cot_all,
        routes_t, tokens, n_total, c_in, n2, probs, h1, qkv, lse, mine, wqkv, wout, gains, router
    )


def per_device(
    tokens,
    cotangent,
    seq_lengths,
    deal,
    routes,
    attn_qkv,
    qkv_first,
    qkv_second,
    attn_out,
    out_first,
    out_second,
    rel_bias,
    bias_first,
    bias_second,
    router,
    router_first,
    router_second,
    norm_gains,
    gains_first,
    gains_second,
    expert_in,
    in_first,
    in_second,
    expert_out,
    down_first,
    down_second,
):
    rows, width = tokens.shape
    experts = router.shape[1]
    capacity = (10 * rows + 4 * experts - 1) // (4 * experts)
    exps = lax.axis_size("exp")
    grps = lax.axis_size("grp")
    routes_t = routes.T
    bias_table = rel_bias.T
    (
        both_w, down_w, cot_all, n_all, comb_all, qkv, lse, context_mine, normed_group, wqkv, wout, hidden_one,
        normed_two, router_probs, in_low, down_low,
    ) = forward_call(
        grps, exps, seq_lengths, bias_table, routes_t, tokens, cotangent, norm_gains.T, router.T,
        attn_qkv, attn_out, expert_in[0], expert_out[0],
    )
    n_total, y_half, y_far, c_in, both_g, down_g, in_before, down_before = expert_call(
        grps, exps, capacity, deal, routes_t, comb_all, n_all, cot_all, both_w, down_w, in_low, down_low,
        hidden_one,
    )
    token_grad, block_out, in_parts, down_parts, qkv_grad, out_grad, small = backward_call(
        grps, exps, seq_lengths, deal, bias_table, y_half, y_far, both_g, down_g,
        in_before, down_before, normed_group, cot_all, routes_t, tokens, n_total, c_in, normed_two, router_probs, hidden_one, qkv, lse, context_mine, wqkv,
        wout, norm_gains.T, router.T,
    )
    states = [
        attn_qkv, qkv_first, qkv_second, attn_out, out_first, out_second, bias_table, bias_first.T, bias_second.T,
        router.T, router_first.T, router_second.T, norm_gains.T, gains_first.T, gains_second.T,
        expert_in[0], in_first[0], in_second[0], expert_out[0], down_first[0], down_second[0],
    ]
    new = list(adam_call(exps, in_parts, down_parts, qkv_grad, out_grad, small, states))
    new = new[:6] + [array.T for array in new[6:15]] + [array[None] for array in new[15:]]
    return (block_out, token_grad, *new)


def bucket_onehot(length):
    places = jnp.arange(length, dtype=jnp.int32)
    offset = places[None, :] - places[:, None]
    distance = jnp.abs(offset)
    bucket = 16 * (offset > 0).astype(jnp.int32)
    for threshold in thresholds:
        bucket = bucket + (distance >= threshold).astype(jnp.int32)
    return (bucket[:, :, None] == jnp.arange(BUCKETS, dtype=jnp.int32)[None, None, :]).astype(full)


def swap(pieces, axes):
    return lax.all_to_all(pieces, axes, split_axis=0, concat_axis=0, tiled=True)


def spread(block, axes):
    members = lax.axis_size(axes)
    return swap(jnp.broadcast_to(block[None], (members,) + block.shape), axes)


def plain_device(
    tokens,
    cotangent,
    seq_lengths,
    deal,
    routes,
    attn_qkv,
    qkv_first,
    qkv_second,
    attn_out,
    out_first,
    out_second,
    rel_bias,
    bias_first,
    bias_second,
    router,
    router_first,
    router_second,
    norm_gains,
    gains_first,
    gains_second,
    expert_in,
    in_first,
    in_second,
    expert_out,
    down_first,
    down_second,
):
    rows, width = tokens.shape
    head_dim = width // HEADS
    score_scale = 1.0 / math.sqrt(head_dim)
    experts = router.shape[1]
    capacity = (10 * rows + 4 * experts - 1) // (4 * experts)
    exps = lax.axis_size("exp")
    grps = lax.axis_size("grp")
    reps = grps * QUAD
    heads = HEADS // exps
    head_cols = heads * head_dim
    place = lax.axis_index("exp")
    base = lax.axis_index(REP) * exps
    me = base + place
    slab = expert_in.shape[1]
    units = expert_out.shape[1]
    quarter = grps * units

    row_block = attn_qkv.shape[0]
    qkv_rows = lax.all_gather(attn_qkv.astype(low), REP, axis=1, tiled=True)
    out_rows = lax.all_gather(attn_out.astype(low), REP, axis=1, tiled=True)
    qkv_pieces = jnp.transpose(
        qkv_rows.reshape(row_block, 3, exps, head_cols), (2, 0, 1, 3)
    ).reshape(exps, row_block, 3 * head_cols)
    qkv_mine = swap(qkv_pieces, "exp").reshape(width, 3 * head_cols)
    full_out = spread(out_rows, "exp").reshape(width, width)

    group_tokens = spread(tokens, "exp")
    group_cotangent = spread(cotangent, "exp")
    my_cotangent = lax.dynamic_index_in_dim(group_cotangent, deal[me] - base, 0, keepdims=False)

    my_routes = lax.dynamic_slice_in_dim(routes, me * rows, rows, 0)
    places = jnp.arange(rows, dtype=jnp.int32)
    valid_rows = (places < seq_lengths[me]).astype(full)
    group_lengths = lax.dynamic_slice_in_dim(seq_lengths, base, exps, 0)
    key_ok = places[None, :] < group_lengths[:, None]
    gain_one = norm_gains[:, 0]
    gain_two = norm_gains[:, 1]

    chosen = (my_routes[:, :, None] == jnp.arange(experts, dtype=jnp.int32)[None, None, :]).astype(full)
    flat_routes = my_routes.reshape(-1)
    route_hot = (flat_routes[:, None] == jnp.arange(experts, dtype=jnp.int32)[None, :]).astype(jnp.int32)
    before = jnp.cumsum(route_hot, axis=0) - route_hot
    slot_index = jnp.sum(before * route_hot, axis=-1)
    target = (flat_routes * capacity + slot_index).reshape(rows, 2)
    slots = experts * capacity
    slot_ids = jnp.arange(slots, dtype=jnp.int32)
    place_first = slot_ids[:, None] == target[None, :, 0]
    place_second = slot_ids[:, None] == target[None, :, 1]
    place_any = jnp.logical_or(place_first, place_second).astype(low)

    shard_in = expert_in[0].astype(low).reshape(slab, 2, grps, QUAD, units)
    in_pieces = jnp.transpose(shard_in, (1, 3, 0, 2, 4)).reshape(2, 1, QUAD, slab, quarter)
    in_pieces = jnp.broadcast_to(in_pieces, (2, grps, QUAD, slab, quarter)).reshape(
        2, reps, slab, quarter
    )
    down_mine = spread(expert_out[0].astype(low), "grp").reshape(quarter, width)
    gate_mine = swap(in_pieces[0], REP).reshape(width, quarter)
    up_mine = swap(in_pieces[1], REP).reshape(width, quarter)

    upstream = my_cotangent.astype(full) * valid_rows[:, None]

    def to_experts(block):
        sent = block.reshape((1, experts) + block.shape[1:])
        sent = jnp.broadcast_to(sent, (QUAD,) + sent.shape[1:])
        return swap(sent.reshape((QUAD * experts,) + block.shape[1:]), PLANE)

    def dispatch(values):
        return dot(place_any, values).astype(low).reshape(experts, capacity, width)

    expert_upstream = to_experts(dispatch(upstream.astype(low))).reshape(-1, width)
    active_grad_bare = lax.dot_general(
        expert_upstream, down_mine, (((1,), (1,)), ((), ())), preferred_element_type=full
    )

    x_group = group_tokens.astype(full)
    scale_group = lax.rsqrt(jnp.mean(x_group * x_group, axis=-1, keepdims=True) + eps_norm)
    normed_group = (x_group * scale_group * gain_one).astype(low).reshape(exps * rows, width)
    qkv = dot(normed_group, qkv_mine).astype(low).reshape(exps, rows, 3, heads, head_dim)
    queries = qkv[:, :, 0]
    key_rows = qkv[:, :, 1]
    values = qkv[:, :, 2]
    onehot = bucket_onehot(rows)
    bias_mine = lax.dynamic_slice_in_dim(rel_bias, place * heads, heads, 1)
    bias_table = jnp.einsum("ijb,bh->hij", onehot, bias_mine, precision=highest)

    def scores_of():
        raw = (
            jnp.einsum("sihd,sjhd->shij", queries, key_rows, preferred_element_type=full)
            * score_scale
            + bias_table[None]
        )
        return jnp.where(key_ok[:, None, None, :], raw, -1e30)

    scores = scores_of()
    row_max = jnp.max(scores, axis=-1, keepdims=True)
    log_total = row_max + jnp.log(jnp.sum(jnp.exp(scores - row_max), axis=-1, keepdims=True))
    weights_low = jnp.exp(scores - log_total).astype(low)
    context_mine = (
        jnp.einsum("shij,sjhd->sihd", weights_low, values, preferred_element_type=full)
        .astype(low)
        .reshape(exps, rows, head_cols)
    )
    context = jnp.transpose(swap(context_mine, "exp"), (1, 0, 2)).reshape(rows, width)

    x_float = tokens.astype(full)
    scale_one = lax.rsqrt(jnp.mean(x_float * x_float, axis=-1, keepdims=True) + eps_norm)
    hidden_one = x_float + dot(context, full_out)
    scale_two = lax.rsqrt(jnp.mean(hidden_one * hidden_one, axis=-1, keepdims=True) + eps_norm)
    normed_two = (hidden_one * scale_two * gain_two).astype(low)
    normed_float = normed_two.astype(full)
    router_probs = jax.nn.softmax(jnp.dot(normed_float, router, precision=highest), axis=-1)
    picked = jnp.sum(router_probs[:, None, :] * chosen, axis=-1)
    gate_total = jnp.sum(picked, axis=-1, keepdims=True)
    gate_value = picked / gate_total
    combine = gate_value * valid_rows[:, None]
    combine_slots = jnp.sum(
        jnp.where(place_first, combine[None, :, 0], 0.0)
        + jnp.where(place_second, combine[None, :, 1], 0.0),
        axis=1,
    ).reshape(experts, 1, capacity)

    expert_rows = to_experts(dispatch(normed_two)).reshape(-1, width)
    expert_combine = to_experts(combine_slots).reshape(-1, 1)

    gate_part = dot(expert_rows, gate_mine)
    up_part = dot(expert_rows, up_mine)
    active_float, active_pull = jax.vjp(gated_unit, gate_part, up_part)
    active = active_float.astype(low)
    active_scaled = (active_float * expert_combine).astype(low)
    combine_grad_part = jnp.sum(active_float * active_grad_bare, axis=-1).reshape(
        QUAD * experts, 1, capacity
    )
    gate_part_grad, up_part_grad = active_pull(active_grad_bare * expert_combine)
    gate_part_grad = gate_part_grad.astype(low)
    up_part_grad = up_part_grad.astype(low)
    rows_grad_part = (
        lax.dot_general(gate_part_grad, gate_mine, (((1,), (1,)), ((), ())), preferred_element_type=full)
        + lax.dot_general(up_part_grad, up_mine, (((1,), (1,)), ((), ())), preferred_element_type=full)
    ).astype(low)
    output_part = dot(active, down_mine).astype(low)

    combine_grad_back = swap(combine_grad_part, PLANE)
    rows_grad_back = swap(rows_grad_part.reshape(QUAD * experts, capacity, width), PLANE)
    output_back = swap(output_part.reshape(QUAD * experts, capacity, width), PLANE)

    def transposed_dot(a, b):
        return lax.dot_general(a, b, (((0,), (0,)), ((), ())), preferred_element_type=full)

    down_grad = transposed_dot(active_scaled, expert_upstream).astype(low)
    gate_grad = transposed_dot(expert_rows, gate_part_grad).astype(low)
    up_grad = transposed_dot(expert_rows, up_part_grad).astype(low)
    down_share = jnp.sum(
        swap(down_grad.reshape(grps, units, width), "grp").astype(full), axis=0
    )[None]

    def in_columns(grad):
        back = swap(grad.reshape(reps, slab, quarter), REP).astype(full)
        back = jnp.sum(back.reshape(grps, QUAD, slab, grps, units), axis=0)
        return jnp.transpose(back, (1, 2, 0, 3)).reshape(slab, grps * QUAD * units)

    in_share = jnp.concatenate([in_columns(gate_grad), in_columns(up_grad)], axis=1)[None]

    def from_slots(placed, parts):
        hot = jnp.broadcast_to(placed.astype(low)[None], (QUAD,) + placed.shape).reshape(-1, rows)
        return lax.dot_general(
            hot, parts.reshape(-1, width), (((0,), (0,)), ((), ())), preferred_element_type=full
        )

    mixture = combine[:, :1] * from_slots(place_first, output_back) + combine[:, 1:] * from_slots(
        place_second, output_back
    )
    block_loader = (valid_rows[:, None] * (hidden_one + mixture)).astype(low)
    seq_ids = jnp.arange(deal.shape[0], dtype=jnp.int32)
    dealt_seq = jnp.sum(jnp.where(deal == me, seq_ids, 0))
    block_out = lax.dynamic_index_in_dim(
        spread(block_loader, "exp"), dealt_seq - base, 0, keepdims=False
    )

    combine_grad_slots = jnp.sum(combine_grad_back.reshape(QUAD, slots), axis=0)
    combine_grad = jnp.stack(
        [
            jnp.sum(jnp.where(place_first, combine_grad_slots[:, None], 0.0), axis=0),
            jnp.sum(jnp.where(place_second, combine_grad_slots[:, None], 0.0), axis=0),
        ],
        axis=1,
    )
    gate_grad_value = combine_grad * valid_rows[:, None]
    picked_grad = (
        gate_grad_value - jnp.sum(gate_grad_value * gate_value, axis=-1, keepdims=True)
    ) / gate_total
    probs_grad = jnp.sum(picked_grad[:, :, None] * chosen, axis=1)
    logit_grad = router_probs * (
        probs_grad - jnp.sum(probs_grad * router_probs, axis=-1, keepdims=True)
    )
    router_grad = jnp.dot(normed_float.T, logit_grad, precision=highest)
    normed_grad = jnp.dot(logit_grad, router.T, precision=highest) + from_slots(
        jnp.logical_or(place_first, place_second), rows_grad_back
    )
    scaled_two = normed_grad * gain_two
    hidden_grad = (
        upstream
        + scale_two * scaled_two
        - hidden_one * scale_two**3 * jnp.mean(scaled_two * hidden_one, axis=-1, keepdims=True)
    )
    gain_two_grad = jnp.sum(normed_grad * hidden_one * scale_two, axis=0)
    branch_grad = hidden_grad.astype(low)
    context_grad = lax.dot_general(
        branch_grad, full_out, (((1,), (1,)), ((), ())), preferred_element_type=full
    ).astype(low)
    context_grad_pieces = jnp.transpose(context_grad.reshape(rows, exps, head_cols), (1, 0, 2))
    context_grad_mine = swap(context_grad_pieces, "exp").reshape(exps, rows, heads, head_dim)
    branch_group = spread(branch_grad, "exp").reshape(exps * rows, width)
    out_grad = transposed_dot(context_mine.reshape(exps * rows, head_cols), branch_group).astype(low)

    scores = scores_of()
    probs_again = jnp.exp(scores - log_total)
    weights_again = probs_again.astype(low)
    values_grad = jnp.einsum(
        "shij,sihd->sjhd", weights_again, context_grad_mine, preferred_element_type=full
    )
    probs_grad_att = jnp.einsum(
        "sihd,sjhd->shij", context_grad_mine, values, preferred_element_type=full
    )
    row_delta = jnp.sum(probs_grad_att * probs_again, axis=-1, keepdims=True)
    scores_grad = (probs_again * (probs_grad_att - row_delta)).astype(low)
    scores_grad_sum = jnp.sum(scores_grad.astype(full), axis=0)
    bias_grad_mine = jnp.einsum("hij,ijb->bh", scores_grad_sum, onehot, precision=highest)
    bias_grad = lax.dynamic_update_slice_in_dim(
        jnp.zeros((BUCKETS, HEADS), full), bias_grad_mine, place * heads, 1
    )
    queries_grad = (
        jnp.einsum("shij,sjhd->sihd", scores_grad, key_rows, preferred_element_type=full)
        * score_scale
    )
    keys_grad = (
        jnp.einsum("shij,sihd->sjhd", scores_grad, queries, preferred_element_type=full)
        * score_scale
    )
    qkv_grad = (
        jnp.stack([queries_grad, keys_grad, values_grad], axis=2)
        .astype(low)
        .reshape(exps * rows, 3 * head_cols)
    )
    normed_one_part = lax.dot_general(
        qkv_grad, qkv_mine, (((1,), (1,)), ((), ())), preferred_element_type=full
    ).astype(low)
    normed_one_grad = jnp.sum(
        swap(normed_one_part.reshape(exps, rows, width), "exp").astype(full), axis=0
    )
    scaled_one = normed_one_grad * gain_one
    token_grad = (
        hidden_grad
        + scale_one * scaled_one
        - x_float * scale_one**3 * jnp.mean(scaled_one * x_float, axis=-1, keepdims=True)
    )
    gain_one_grad = jnp.sum(normed_one_grad * x_float * scale_one, axis=0)

    qkv_weight_grad = transposed_dot(normed_group, qkv_grad).astype(low)
    qkv_grad_rows = swap(qkv_weight_grad.reshape(exps, row_block, 3 * head_cols), "exp")
    qkv_grad_rows = jnp.transpose(
        qkv_grad_rows.reshape(exps, row_block, 3, head_cols), (1, 2, 0, 3)
    ).reshape(row_block, reps, -1)
    qkv_share = jnp.sum(
        swap(jnp.transpose(qkv_grad_rows, (1, 0, 2)), REP).astype(full), axis=0
    )
    out_pieces = jnp.transpose(out_grad.reshape(row_block, reps, -1), (1, 0, 2))
    out_share = jnp.sum(swap(out_pieces, REP).astype(full), axis=0)

    small = jnp.concatenate(
        [
            router_grad.reshape(-1),
            jnp.stack([gain_one_grad, gain_two_grad], axis=1).reshape(-1),
            bias_grad.reshape(-1),
        ]
    ).reshape(-1, 128)
    small_total = jnp.sum(lax.all_gather(small, ALL, axis=0, tiled=False), axis=0).reshape(-1)
    router_total = small_total[: router.size].reshape(router.shape)
    gains_total = small_total[router.size : router.size + norm_gains.size].reshape(norm_gains.shape)
    bias_total = small_total[router.size + norm_gains.size :].reshape(rel_bias.shape)

    qkv_new = adamw_update(attn_qkv, qkv_first, qkv_second, qkv_share, 1.5 / math.sqrt(D), 0.1)
    out_new = adamw_update(attn_out, out_first, out_second, out_share, 6.0 / math.sqrt(D), 0.1)
    bias_new = adamw_update(rel_bias, bias_first, bias_second, bias_total, 0.3, 0.0)
    router_new = adamw_update(
        router, router_first, router_second, router_total, 1.0 / math.sqrt(D), 0.1
    )
    gains_new = adamw_update(norm_gains, gains_first, gains_second, gains_total, 0.5, 0.0)
    in_new = adamw_update(expert_in, in_first, in_second, in_share, 1.5 / math.sqrt(D), 0.1)
    down_new = adamw_update(
        expert_out, down_first, down_second, down_share, 1.5 / math.sqrt(FF), 0.1
    )
    return (
        (block_out, token_grad)
        + qkv_new
        + out_new
        + bias_new
        + router_new
        + gains_new
        + in_new
        + down_new
    )


def solution(mesh):
    reps, exps = mesh.devices.shape
    split = Mesh(mesh.devices.reshape(reps // QUAD, QUAD, exps), ALL)
    by_rows = P(ALL, None)
    attn = P("exp", REP)
    expert = P("exp", REP, None)
    return jax.shard_map(
        per_device if (reps, exps) == (2 * QUAD, 4) else plain_device,
        mesh=split,
        in_specs=(by_rows, by_rows) + (P(),) * 3 + (attn,) * 6 + (P(),) * 9 + (expert,) * 6,
        out_specs=(by_rows, by_rows) + (attn,) * 6 + (P(),) * 9 + (expert,) * 6,
        check_vma=False,
    )
```

```python
import functools
import math

import jax
import jax.numpy as jnp
from jax import lax
from jax.experimental import pallas as pl
from jax.experimental.pallas import tpu as pltpu
from jax.sharding import Mesh
from jax.sharding import PartitionSpec as P

D = 1024
HEADS = 16
FF = 2816
BUCKETS = 32
STEP = 10
QUAD = 4
REP = ("grp", "quad")
PLANE = ("quad", "exp")
ALL = ("grp", "quad", "exp")

highest = lax.Precision.HIGHEST
eps_norm = 1e-06
thresholds = (1, 2, 3, 4, 5, 6, 7, 8, 11, 16, 22, 32, 45, 64, 90)
beta_one = 0.9
beta_two = 0.999
eps_adam = 1e-08
low = jnp.bfloat16
full = jnp.float32
MESH = pl.DeviceIdType.MESH


def adamw_update(weight, moment, second, gradient, step_rate, decay_factor):
    new_moment = beta_one * moment + (1.0 - beta_one) * gradient
    new_second = beta_two * second + (1.0 - beta_two) * gradient * gradient
    corrected = new_moment / (1.0 - beta_one**STEP)
    scaled = new_second / (1.0 - beta_two**STEP)
    new_weight = weight - step_rate * (
        corrected / (jnp.sqrt(scaled) + eps_adam) + decay_factor * weight
    )
    return (new_moment, new_second, new_weight)


def gated_unit(gate_input, up_input):
    return jax.nn.gelu(gate_input, approximate=True) * up_input


def dot(a, b):
    return jnp.dot(a, b, preferred_element_type=full)


def nt(a, b, precision=None):
    return lax.dot_general(a, b, (((1,), (1,)), ((), ())), preferred_element_type=full, precision=precision)


def tn(a, b):
    return lax.dot_general(a, b, (((0,), (0,)), ((), ())), preferred_element_type=full)


class Where:
    def __init__(self, grps, exps):
        self.grps, self.exps = grps, exps
        self.reps = grps * QUAD
        self.grp = lax.axis_index("grp")
        self.quad = lax.axis_index("quad")
        self.exp = lax.axis_index("exp")
        self.rep = self.grp * QUAD + self.quad
        self.base = self.rep * exps
        self.me = self.base + self.exp

    def device(self, rep, exp):
        return (rep // QUAD, rep % QUAD, exp)

    def near(self, flip):
        q = self.quad
        if flip & 1:
            q = q + 1 - 2 * (q % 2)
        if flip & 2:
            q = q + 2 - 4 * (q // 2)
        return q


def send(src, dst, send_sem, recv_sem, device):
    return pltpu.make_async_remote_copy(
        src_ref=src, dst_ref=dst, send_sem=send_sem, recv_sem=recv_sem, device_id=device, device_id_type=MESH
    )


def arrived(ref, sem):
    pltpu.make_async_copy(ref, ref, sem).wait()


def greet(count, device):
    barrier = pltpu.get_barrier_semaphore()

    def one(k, _):
        pl.semaphore_signal(barrier, inc=1, device_id=device(k), device_id_type=MESH)
        return 0

    lax.fori_loop(1, count + 1, one, 0)
    return functools.partial(pl.semaphore_wait, barrier, count)


def everyone(at):
    count = at.reps * at.exps

    def device(k):
        other = (at.me + k) % count
        return at.device(other // at.exps, other % at.exps)

    return count - 1, device


def neighbours(at):
    members = QUAD * at.exps
    plane = at.quad * at.exps + at.exp

    def device(k):
        other = (plane + k) % members
        rest = k - members
        grp = jnp.where(k < members, at.grp, (at.grp + 1 + rest // QUAD) % at.grps)
        quad = jnp.where(k < members, other // at.exps, rest % QUAD)
        return grp, quad, jnp.where(k < members, other % at.exps, at.exp)

    return members - 1 + QUAD * (at.grps - 1), device


def turn(exp, i):
    beside = exp + 1 - 2 * (exp % 2)
    return jnp.where(i == 0, (beside + 2) % 4, jnp.where(i == 1, (exp + 2) % 4, jnp.where(i == 2, beside, exp)))


def lane_of(shape):
    return lax.broadcasted_iota(jnp.int32, shape, 1)


def row_of(shape):
    return lax.broadcasted_iota(jnp.int32, shape, 0)


def bucket_of(offset):
    distance = jnp.abs(offset)
    bucket = jnp.where(offset > 0, 16, 0)
    for threshold in thresholds:
        bucket = bucket + jnp.where(distance >= threshold, 1, 0)
    return bucket


def bits_of(count):
    return count.bit_length() - 1


def column_parts(width):
    tiles = width // 128
    cuts = [0, (tiles + 2) // 3, (2 * tiles + 2) // 3, tiles]
    return [(cuts[i] * 128, (cuts[i + 1] - cuts[i]) * 128) for i in range(3)]


def flipped(place, bit):
    return place + (1 - 2 * ((place // (1 << bit)) % 2)) * (1 << bit)


class Doubling:
    def __init__(self, at, own, every, sems, core_sems, orders):
        self.at, self.own, self.every = at, own, every
        self.sems, self.core_sems, self.orders = sems, core_sems, orders
        self.plane = at.quad * at.exps + at.exp
        self.steps = len(orders[0])
        self.parts = column_parts(own.shape[1])

    def device(self, bit):
        other = flipped(self.plane, bit)
        return (self.at.grp, other // self.at.exps, other % self.at.exps)

    def place(self, part, j):
        p = self.plane
        for i, bit in enumerate(self.orders[part]):
            if (j >> i) & 1:
                p = flipped(p, bit + 1)
        return p

    def block(self, part, p):
        begin, size = self.parts[part]
        return self.every.at[p, :, pl.ds(begin, size)]

    def source(self, part, j):
        begin, size = self.parts[part]
        return self.own.at[:, pl.ds(begin, size)] if j == 0 else self.block(part, self.place(part, j))

    def index(self, step, part, j):
        return part * (1 << self.steps) + (1 << step) - 1 + j

    def copy(self, step, part, j):
        i = self.index(step, part, j)
        return send(
            self.source(part, j),
            self.block(part, self.place(part, j)),
            self.sems.at[0, i],
            self.sems.at[1, i],
            self.device(self.orders[part][step] + 1),
        )

    def core_copy(self, part, j):
        i = part * (1 << self.steps) + j
        return send(
            self.source(part, j),
            self.block(part, self.place(part, j)),
            self.core_sems.at[0, i],
            self.core_sems.at[1, i],
            self.device(0),
        )

    def start(self):
        for part in range(3):
            for step in range(self.steps):
                self.copy(step, part, 0).start()
        for part in range(3):
            self.core_copy(part, 0).start()
        self.keep().start()

    def keep(self):
        return pltpu.make_async_copy(self.own, self.every.at[self.plane], self.core_sems.at[1, 3 << self.steps])

    def next(self, step):
        for part in range(3):
            for j in range(1 << step):
                k = (1 << step) + j
                arrived(self.block(part, self.place(part, k)), self.sems.at[1, self.index(step, part, j)])
                for later in range(step + 1, self.steps):
                    self.copy(later, part, k).start()
                self.core_copy(part, k).start()

    def finish_in(self):
        for part in range(3):
            for j in range(1 << self.steps):
                there = self.block(part, flipped(self.place(part, j), 0))
                arrived(there, self.core_sems.at[1, part * (1 << self.steps) + j])
        self.keep().wait()

    def finish_out(self):
        for part in range(3):
            for j in range(1 << self.steps):
                self.core_copy(part, j).wait_send()
            for step in range(self.steps):
                for j in range(1 << step):
                    self.copy(step, part, j).wait_send()


class Halving:
    def __init__(self, at, bufs, sems, orders):
        self.at, self.bufs, self.sems = at, bufs, sems
        self.plane = at.quad * at.exps + at.exp
        self.places = bits_of(QUAD * at.exps)
        self.chip_bits = list(range(self.places - 1))
        self.parts = column_parts(bufs[0].shape[2])
        self.orders = orders

    def device(self, bit):
        other = flipped(self.plane, bit)
        return (self.at.grp, other // self.at.exps, other % self.at.exps)

    def hop(self, step, part):
        order = self.orders[part]
        bit = order[step]
        left = [b for b in self.chip_bits if b not in order[:step]]
        pos = left.index(bit)
        half = 1 << (len(left) - 1)
        mine = (self.plane // (1 << (bit + 1))) % 2
        device = self.device(bit + 1)
        begin, size = self.parts[part]
        cols = pl.ds(begin, size)
        base = self.base(step, part)

        def index(j, value):
            return (j >> pos) * (1 << (pos + 1)) + value * (1 << pos) + j % (1 << pos)

        pairs = []
        for j in range(half):
            copy = functools.partial(
                send,
                self.bufs[step].at[index(j, 1 - mine), :, cols],
                self.bufs[step + 1].at[j, :, cols],
                self.sems.at[0, base + j],
                self.sems.at[1, base + j],
                device,
            )
            pairs.append((copy, index(j, mine), j))
        return pairs, begin, size, base

    def base(self, step, part):
        n = len(self.chip_bits)
        return part * (1 << n) + sum(1 << (n - 1 - s) for s in range(step))

    def start(self, step, part=None):
        for p in range(3) if part is None else [part]:
            for copy, _, _ in self.hop(step, p)[0]:
                copy().start()

    def add(self, step, part):
        pairs, begin, size, base = self.hop(step, part)
        cols = pl.ds(begin, size)
        here, there = self.bufs[step], self.bufs[step + 1]
        for _, keep, j in pairs:
            arrived(there.at[j, :, cols], self.sems.at[1, base + j])
            there[j, :, begin : begin + size] = (
                there[j, :, begin : begin + size] + here[keep, :, begin : begin + size]
            )

    def next(self, step):
        for p in range(3):
            self.add(step, p)
            if step + 1 < len(self.chip_bits):
                self.start(step + 1, p)

    def result(self):
        return self.bufs[len(self.chip_bits)]

    def finish(self):
        for step in range(len(self.chip_bits)):
            for p in range(3):
                for copy, _, _ in self.hop(step, p)[0]:
                    copy().wait_send()


class Group:
    def __init__(self, at, own, every, sems):
        self.at, self.own, self.every, self.sems = at, own, every, sems
        self.beside, self.across = at.exp + 1 - 2 * (at.exp % 2), (at.exp + 2) % 4

    def copy(self, src, index, send_index, device):
        return send(
            src, self.every.at[index], self.sems.at[0, send_index], self.sems.at[1, index], self.at.device(self.at.rep, device)
        )

    def first(self):
        return [
            self.copy(self.own, self.at.exp, 0, self.across),
            self.copy(self.own, self.at.exp, 1, self.beside),
        ]

    def second(self):
        return self.copy(self.every.at[self.across], self.across, 2, self.beside)

    def start(self):
        for copy in self.first():
            copy.start()

    def pass_on(self):
        arrived(self.every.at[self.across], self.sems.at[1, self.across])
        self.second().start()

    def arrive(self):
        for index in (self.beside, (self.beside + 2) % 4):
            arrived(self.every.at[index], self.sems.at[1, index])

    def sent(self):
        for copy in self.first() + [self.second()]:
            copy.wait_send()


class Tiles:
    def __init__(self, units, reps):
        self.units = units
        self.reps = reps
        self.hidden = units * reps
        self.half = self.hidden // 256
        self.wide = (self.half + 1) // 2
        self.count = 3
        self.size = 128 * self.wide // self.count
        self.skip = 128 * (2 * self.wide - self.half)

    def start(self, quad):
        return 128 * (self.half * (quad // 2) + (self.half - self.wide) * (quad % 2))

    def rows(self, tile):
        result = []
        for k in range(QUAD):
            found = None
            for parity in range(2):
                first = self.start(parity) + tile * self.size
                live = first + (self.skip if parity and tile == 0 else 0)
                begin = max(live, k * self.units)
                end = min(first + self.size, (k + 1) * self.units)
                if end > begin:
                    found = (begin - k * self.units, end - begin, parity, begin - first)
            result.append(found)
        return result


class Outward:
    def __init__(self, at, tiles, tile, in_low, down_slab, both_w, down_w, nothing, sems, down_sems):
        self.at, self.tiles, self.tile = at, tiles, tile
        self.in_low, self.down_slab, self.both_w, self.down_w = in_low, down_slab, both_w, down_w
        self.nothing, self.sems, self.down_sems = nothing, sems, down_sems
        self.slab = in_low.shape[0]

    def source(self, quad, section):
        begin = section * self.tiles.hidden + self.tiles.start(quad) + self.tile * self.tiles.size
        return self.in_low.at[:, pl.ds(pl.multiple_of(begin, 128), self.tiles.size)]

    def target(self, rep, section):
        rows = pl.ds(pl.multiple_of(rep * self.slab, self.slab), self.slab)
        return self.both_w.at[rows, pl.ds(section * self.tiles.size, self.tiles.size)]

    def over(self, act):
        at = self.at

        def one(k, _):
            other = (at.rep + k) % at.reps
            for section in range(2):
                act(
                    functools.partial(
                        send,
                        self.source(other % QUAD, section),
                        self.target(at.rep, section),
                        self.sems.at[0, section * at.reps + other],
                        self.sems.at[1, section * at.reps + at.rep],
                        at.device(other, at.exp),
                    )
                )
            return 0

        lax.fori_loop(1, at.reps, one, 0)

    def over_down(self, act, act_local):
        at = self.at
        for k, piece in enumerate(self.tiles.rows(self.tile)):
            if piece is None:
                continue
            begin, count, parity, to = piece
            quad = 2 * (at.rep // QUAD) + parity
            src, dst = self.down_slab.at[pl.ds(begin, count)], self.down_w.at[pl.ds(to, count)]
            recv = self.down_sems.at[1, at.rep]
            for g in range(at.grps):
                stays = jnp.logical_and(at.grp == g, at.quad == quad)
                ours = at.rep % QUAD == k

                @pl.when(jnp.logical_and(ours, jnp.logical_not(stays)))
                def _():
                    act(functools.partial(send, src, dst, self.down_sems.at[0, g], recv, (g, quad, at.exp)))

                @pl.when(jnp.logical_and(ours, stays))
                def _():
                    act_local(functools.partial(pltpu.make_async_copy, src, dst, recv))

    def blank(self):
        return pltpu.make_async_copy(
            self.nothing, self.down_w.at[pl.ds(0, self.tiles.skip)], self.down_sems.at[1, self.at.reps]
        )

    def start(self):
        at = self.at
        self.over_down(lambda copy: copy().start(), lambda copy: copy().start())
        self.over(lambda copy: copy().start())
        for section in range(2):
            pltpu.make_async_copy(
                self.source(at.quad, section), self.target(at.rep, section), self.sems.at[1, section * at.reps + at.rep]
            ).start()
        if self.tile == 0:

            @pl.when(at.quad % 2 == 1)
            def _():
                self.blank().start()

    def arrive(self):
        at = self.at

        def one(rep, _):
            for section in range(2):
                arrived(self.target(rep, section), self.sems.at[1, section * at.reps + rep])
            return 0

        lax.fori_loop(0, at.reps, one, 0)
        for parity in range(2):

            @pl.when(at.quad % 2 == parity)
            def _():
                for k, piece in enumerate(self.tiles.rows(self.tile)):
                    if piece is not None and piece[2] == parity:
                        source = QUAD * (at.quad // 2) + k
                        arrived(self.down_w.at[pl.ds(piece[3], piece[1])], self.down_sems.at[1, source])
                if parity and self.tile == 0:
                    self.blank().wait()

    def sent(self):
        self.over(lambda copy: copy().wait_send())
        self.over_down(lambda copy: copy().wait_send(), lambda copy: None)


class Homeward:
    def __init__(self, at, tiles, tile, both, down, in_parts, down_parts, sems, down_sems, sections=(0, 1)):
        self.at, self.tiles, self.tile, self.sections = at, tiles, tile, sections
        self.both, self.down, self.in_parts, self.down_parts = both, down, in_parts, down_parts
        self.sems, self.down_sems = sems, down_sems
        self.slab = in_parts.shape[1]

    def target(self, grp, quad, parity, section):
        skip = self.tiles.skip if parity and self.tile == 0 else 0
        to = section * self.tiles.hidden + self.tiles.start(quad) + self.tile * self.tiles.size + skip
        to = to if isinstance(to, int) else pl.multiple_of(to, 128)
        return skip, self.in_parts.at[grp, :, pl.ds(to, self.tiles.size - skip)]

    def copy(self, rep, parity, section, local=False):
        at = self.at
        skip, dst = self.target(at.grp, at.quad, parity, section)
        rows = pl.ds(pl.multiple_of(rep * self.slab, self.slab), self.slab)
        src = self.both.at[rows, pl.ds(section * self.tiles.size + skip, self.tiles.size - skip)]
        recv = self.sems.at[1, section * at.reps + at.rep]
        if local:
            return pltpu.make_async_copy(src, dst, recv)
        return send(src, dst, self.sems.at[0, section * at.reps + rep], recv, at.device(rep, at.exp))

    def over(self, act, act_local):
        at = self.at
        for parity in range(2):

            @pl.when(at.quad % 2 == parity)
            def _():
                def one(k, _):
                    for section in self.sections:
                        act(self.copy((at.rep + k) % at.reps, parity, section))
                    return 0

                lax.fori_loop(1, at.reps, one, 0)
                if act_local:
                    for section in self.sections:
                        act_local(self.copy(at.rep, parity, section, local=True))

    def over_down(self, act, act_local):
        at = self.at
        if self.down is None:
            return
        for k, piece in enumerate(self.tiles.rows(self.tile)):
            if piece is None:
                continue
            begin, count, parity, to = piece
            src, dst = self.down.at[pl.ds(to, count)], self.down_parts.at[at.grp, pl.ds(begin, count)]
            recv = self.down_sems.at[1, at.grp]
            stays = jnp.logical_and(at.grp == at.quad // 2, at.quad == k)
            ours = at.quad % 2 == parity

            @pl.when(jnp.logical_and(ours, jnp.logical_not(stays)))
            def _():
                act(functools.partial(send, src, dst, self.down_sems.at[0, k], recv, (at.quad // 2, k, at.exp)))

            @pl.when(jnp.logical_and(ours, stays))
            def _():
                act_local(functools.partial(pltpu.make_async_copy, src, dst, recv))

    def start(self):
        self.over_down(lambda copy: copy().start(), lambda copy: copy().start())
        self.over(lambda copy: copy.start(), lambda copy: copy.start())

    def arrive(self):
        at = self.at
        for rep in range(at.reps):
            for section in self.sections:
                _, dst = self.target(rep // QUAD, rep % QUAD, rep % 2, section)
                arrived(dst, self.sems.at[1, section * at.reps + rep])
        for k, piece in enumerate(self.tiles.rows(self.tile)):
            if piece is None or self.down is None:
                continue

            @pl.when(at.quad == k)
            def _():
                for g in range(at.grps):
                    arrived(self.down_parts.at[g, pl.ds(piece[0], piece[1])], self.down_sems.at[1, g])

    def sent(self):
        self.over(lambda copy: copy.wait_send(), None)
        self.over_down(lambda copy: copy().wait_send(), lambda copy: None)


def forward_kernel(
    grps,
    exps,
    lengths,
    bias_table,
    routes_t,
    tokens,
    cotangent,
    gains,
    router,
    attn_qkv,
    attn_out,
    expert_in,
    expert_out,
    both_w,
    down_w,
    cot_all,
    n_all,
    comb_all,
    qkv_out,
    pb_out,
    mine_out,
    n1_out,
    wqkv_out,
    wout_out,
    h1_out,
    n2_out,
    probs_out,
    in_out,
    down_out,
    in_wide,
    down_wide,
    qkv_t,
    out_w,
    in_low,
    down_slab,
    tok_all,
    wqkv,
    wout,
    n1,
    qkv,
    pb,
    mine,
    ctx,
    bias,
    comb_send,
    nothing,
    tok_sem,
    wq_sem,
    pass_sem,
    wo_sem,
    wo2_sem,
    weight_sem,
    down_sem,
    ctx_sem,
    cot_sem,
    cot_core_sem,
    n_sem,
    n_core_sem,
    comb_sem,
    store_sem,
    cast_sem,
):
    at = Where(grps, exps)
    reps = at.reps
    rows, width = tokens.shape
    heads = HEADS // exps
    head_dim = width // HEADS
    head_cols = heads * head_dim
    block_cols = min(128, head_cols)
    shard_cols, row_block = qkv_t.shape
    seg = math.gcd(shard_cols, head_cols)
    segs = shard_cols // seg
    tiles = Tiles(down_slab.shape[0], reps)
    plane = at.quad * exps + at.exp
    members = QUAD * exps
    scale = 1.0 / math.sqrt(head_dim)
    SEND, RECV = 0, 1

    met = greet(*everyone(at))
    wide_copies = [
        pltpu.make_async_copy(expert_in, in_wide, cast_sem.at[0]),
        pltpu.make_async_copy(expert_out, down_wide, cast_sem.at[1]),
    ]
    for copy in wide_copies:
        copy.start()
    qkv_t[...] = attn_qkv[...].T.astype(low)
    out_w[...] = attn_out[...].astype(low)
    met()

    def exp_peer(k):
        return (at.exp + k) % exps

    group_tokens = Group(at, tokens, tok_all, tok_sem)
    group_tokens.start()
    tok_all[at.exp] = tokens[...]

    def segment(k):
        col = (at.rep * segs + k) * seg
        section = col // width
        within = col - section * width
        owner = within // head_cols
        return owner, section * head_cols + within - owner * head_cols

    seg_count = 3 * head_cols // seg

    def segment_copy(k, shift):
        owner, offset = segment(k)
        src = qkv_t.at[pl.ds(k * seg, seg)]
        dst = wqkv.at[at.exp, pl.ds(pl.multiple_of(offset, seg), seg)]
        grp = jnp.where(shift < QUAD, at.grp, (at.grp + shift - QUAD + 1) % grps)
        quad = jnp.where(shift < QUAD, (at.quad + shift) % QUAD, at.quad)
        return owner, src, dst, functools.partial(
            send,
            src,
            dst,
            wq_sem.at[SEND, k * fan + shift],
            wq_sem.at[RECV, at.exp * seg_count + offset // seg],
            (grp, quad, owner),
        )

    fan = QUAD + grps - 1

    def over_segments(act, act_local):
        def one(i, _):
            k, shift = i // fan, i % fan
            owner, src, dst, copy = segment_copy(k, shift)
            stays = jnp.logical_and(shift == 0, owner == at.exp)

            @pl.when(jnp.logical_not(stays))
            def _():
                act(copy())

            @pl.when(stays)
            def _():
                act_local(k, src, dst)

            return 0

        lax.fori_loop(0, segs * fan, one, 0)

    def local_segment(k, src, dst):
        _, offset = segment(k)
        pltpu.make_async_copy(src, dst, wq_sem.at[RECV, at.exp * seg_count + offset // seg]).start()

    over_segments(lambda copy: copy.start(), local_segment)

    def over_passed(act):
        def one(i, _):
            e, j = i // seg_count, i % seg_count
            col = (j // (head_cols // seg)) * width + at.exp * head_cols + (j % (head_cols // seg)) * seg
            rep = col // seg // segs

            @pl.when(jnp.logical_and(rep % QUAD == at.quad, rep != at.rep))
            def _():
                block = wqkv.at[e, pl.ds(pl.multiple_of(j * seg, seg), seg)]
                act(i, block)

            return 0

        lax.fori_loop(0, exps * seg_count, one, 0)

    def passed_copies(i, block):
        return [
            send(
                block,
                block,
                pass_sem.at[i, k - 1],
                wq_sem.at[RECV, i],
                (at.grp, (at.quad + k) % QUAD, at.exp),
            )
            for k in range(1, QUAD)
        ]

    def pass_on(i, block):
        arrived(block, wq_sem.at[RECV, i])
        for copy in passed_copies(i, block):
            copy.start()

    def passed_sent(i, block):
        for copy in passed_copies(i, block):
            copy.wait_send()

    for k in range(1, reps):
        other = (at.rep + k) % reps
        send(
            out_w, wout.at[at.exp, at.rep], wo_sem.at[SEND, other], wo_sem.at[RECV, at.rep], at.device(other, at.exp)
        ).start()
    wout[at.exp, at.rep] = out_w[...]
    chip_bits = list(range(bits_of(members) - 1))
    cots = Doubling(at, cotangent, cot_all, cot_sem, cot_core_sem, [chip_bits[::-1]] * 3)
    cots.start()

    span = 2 * rows
    bucket = bucket_of(lane_of((8, span)) - rows)
    for h in range(heads):
        line = jnp.zeros((8, span), full)
        for b in range(BUCKETS):
            line = jnp.where(bucket == b, bias_table[at.exp * heads + h, b], line)
        whole = jnp.broadcast_to(line[0:1], (rows, span))
        bias[h] = pltpu.roll(whole, 0, 1, stride=1, stride_axis=0)[:, rows:]

    group_tokens.pass_on()
    group_tokens.arrive()

    def norm_group(s, _):
        x = tok_all[s].astype(full)
        r = lax.rsqrt(jnp.mean(x * x, axis=1, keepdims=True) + eps_norm)
        n1[s] = (x * r * gains[0:1, :]).astype(low)
        return 0

    lax.fori_loop(0, exps, norm_group, 0)

    over_passed(pass_on)

    for copy in wide_copies:
        copy.wait()
    in_low[...] = in_wide[...].astype(low)
    down_slab[...] = down_wide[...].astype(low)
    nothing[...] = jnp.zeros_like(nothing)
    weights = [
        Outward(
            at, tiles, t, in_low, down_slab, both_w.at[t], down_w.at[t], nothing, weight_sem.at[t], down_sem.at[t]
        )
        for t in range(2)
    ]
    weights[0].start()

    def wait_segment(i, _):
        e, j = i // seg_count, i % seg_count
        col = (j // (head_cols // seg)) * width + at.exp * head_cols + (j % (head_cols // seg)) * seg
        rep = col // seg // segs

        @pl.when(jnp.logical_not(jnp.logical_and(rep % QUAD == at.quad, rep != at.rep)))
        def _():
            arrived(wqkv.at[e, pl.ds(pl.multiple_of(j * seg, seg), seg)], wq_sem.at[RECV, i])

        return 0

    lax.fori_loop(0, exps * seg_count, wait_segment, 0)

    def project(s, _):
        total = jnp.zeros((rows, 3 * head_cols), full)
        for e in range(exps):
            total = total + nt(n1[s, :, e * row_block : (e + 1) * row_block], wqkv[e])
        qkv[s] = total.astype(low)
        return 0

    lax.fori_loop(0, exps, project, 0)

    group_wout = Group(at, wout.at[at.exp], wout, wo2_sem)

    def beside(k):
        if k == 1:
            for j in range(1, reps):
                other = (at.rep + j) % reps
                arrived(wout.at[at.exp, other], wo_sem.at[RECV, other])
            group_wout.start()
        elif k == 2:
            cots.next(0)
        else:
            group_wout.pass_on()

    def attend(i, _):
        s = turn(at.exp, i)
        for k in range(1, exps):

            @pl.when(i == k)
            def _():
                beside(k)

        ok = lane_of((rows, rows)) < lengths[at.base + s]
        lane = lane_of((rows, block_cols))
        for c in range(head_cols // block_cols):
            cols = slice(c * block_cols, (c + 1) * block_cols)
            q = qkv[s, :, cols] * scale
            k = qkv[s, :, head_cols + c * block_cols : head_cols + (c + 1) * block_cols]
            v = qkv[s, :, 2 * head_cols + c * block_cols : 2 * head_cols + (c + 1) * block_cols]
            result = jnp.zeros((rows, block_cols), full)
            for t in range(block_cols // head_dim):
                h = c * (block_cols // head_dim) + t
                here = jnp.logical_and(lane >= t * head_dim, lane < (t + 1) * head_dim)
                scores = nt(jnp.where(here, q, jnp.zeros_like(q)), k) + bias[h]
                scores = jnp.where(ok, scores, -1e30)
                top = jnp.max(scores, axis=1, keepdims=True)
                weights = jnp.exp(scores - top)
                total = jnp.sum(weights, axis=1, keepdims=True)
                weights = (weights * (1.0 / total)).astype(low)
                result = jnp.where(here, jnp.dot(weights, v, preferred_element_type=full), result)
                pb[s * heads + h] = weights
            mine[s, :, cols] = result.astype(low)

        @pl.when(i < exps - 1)
        def _():
            send(
                mine.at[s], ctx.at[at.exp], ctx_sem.at[SEND, s], ctx_sem.at[RECV, at.exp], at.device(at.rep, s)
            ).start()

        @pl.when(i == exps - 1)
        def _():
            pltpu.make_async_copy(mine.at[s], ctx.at[at.exp], ctx_sem.at[RECV, at.exp]).start()

        return 0

    lax.fori_loop(0, exps, attend, 0)

    cots.next(1)
    group_wout.arrive()
    for e in range(exps):
        arrived(ctx.at[e], ctx_sem.at[RECV, e])

    out_cols = wout.shape[3]
    for r in range(reps):
        cols = slice(r * out_cols, (r + 1) * out_cols)
        total = tokens[:, cols].astype(full)
        for e in range(exps):
            total = total + jnp.dot(ctx[e], wout[e, r], preferred_element_type=full)
        h1_out[:, cols] = total
    h1 = h1_out[...]
    r2 = lax.rsqrt(jnp.mean(h1 * h1, axis=1, keepdims=True) + eps_norm)
    n2 = (h1 * r2 * gains[1:2, :]).astype(low)
    n2_out[...] = n2
    rotated = [chip_bits[c:] + chip_bits[:c] for c in range(3)]
    rows_two = Doubling(at, n2_out, n_all, n_sem, n_core_sem, rotated)
    rows_two.start()
    weights[1].start()

    router_rows = jnp.concatenate([router[...], jnp.zeros((128 - exps, width), full)], axis=0)
    logits = nt(n2.astype(full), router_rows, precision=highest)
    lane = lane_of((rows, 128))
    logits = jnp.where(lane < exps, logits, -1e30)
    probs = jnp.exp(logits - jnp.max(logits, axis=1, keepdims=True))
    probs = probs / jnp.sum(probs, axis=1, keepdims=True)
    probs_out[...] = probs
    picked = jnp.where(routed(routes_t, at.me, rows), probs, 0.0)
    comb = picked / jnp.sum(picked, axis=1, keepdims=True)
    comb = jnp.where(row_of((rows, 1)) < lengths[at.me], comb, 0.0)
    comb_send[...] = comb.T[0 : comb_send.shape[0]]

    def comb_copy(k):
        other = (plane + k) % members
        return send(
            comb_send,
            comb_all.at[plane],
            comb_sem.at[SEND, other],
            comb_sem.at[RECV, plane],
            (at.grp, other // exps, other % exps),
        )

    def start_comb(k, _):
        comb_copy(k).start()
        return 0

    lax.fori_loop(1, members, start_comb, 0)
    pltpu.make_async_copy(comb_send, comb_all.at[plane], comb_sem.at[RECV, plane]).start()
    rows_two.next(0)

    stores = [
        (qkv, qkv_out),
        (pb, pb_out),
        (mine, mine_out),
        (n1, n1_out),
        (wqkv, wqkv_out),
        (wout, wout_out),
        (in_low, in_out),
        (down_slab, down_out),
    ]
    for i, (src, dst) in enumerate(stores):
        pltpu.make_async_copy(src, dst, store_sem.at[i]).start()

    for step in range(1, rows_two.steps):
        rows_two.next(step)
    for step in range(2, cots.steps):
        cots.next(step)

    cots.finish_in()
    rows_two.finish_in()

    def comb_in(k, _):
        arrived(comb_all.at[k], comb_sem.at[RECV, k])
        return 0

    lax.fori_loop(0, members, comb_in, 0)
    for tile in weights:
        tile.arrive()

    for k in range(1, exps):
        peer = exp_peer(k)
        arrived(mine.at[peer], ctx_sem.at[SEND, peer])
    over_segments(lambda copy: copy.wait_send(), lambda k, src, dst: None)
    over_passed(passed_sent)
    for k in range(1, reps):
        arrived(out_w, wo_sem.at[SEND, (at.rep + k) % reps])
    group_tokens.sent()
    group_wout.sent()
    cots.finish_out()
    rows_two.finish_out()

    def sent_comb(k, _):
        comb_copy(k).wait_send()
        return 0

    lax.fori_loop(1, members, sent_comb, 0)
    for tile in weights:
        tile.sent()
    for i, (src, dst) in enumerate(stores):
        pltpu.make_async_copy(src, dst, store_sem.at[i]).wait()


def forward_call(
    grps, exps, lengths, bias_table, routes_t, tokens, cotangent, gains, router, attn_qkv, attn_out, expert_in, expert_out
):
    reps = grps * QUAD
    rows, width = tokens.shape
    head_cols = width // exps
    row_block, shard_cols = attn_qkv.shape
    seg = math.gcd(shard_cols, head_cols)
    segs = shard_cols // seg
    units = expert_out.shape[0]
    out_cols = attn_out.shape[1]
    heads = HEADS // exps
    members = QUAD * exps
    tiles = Tiles(units, reps)
    shape = jax.ShapeDtypeStruct
    vmem = pl.BlockSpec(memory_space=pltpu.VMEM)
    smem = pl.BlockSpec(memory_space=pltpu.SMEM)
    hbm = pl.BlockSpec(memory_space=pl.ANY)
    results = [
        (shape((2, width, 2 * tiles.size), low), hbm),
        (shape((2, tiles.size, width), low), hbm),
        (shape((members, rows, width), low), hbm),
        (shape((members, rows, width), low), hbm),
        (shape((members, 8, rows), full), hbm),
        (shape((exps, rows, 3 * head_cols), low), hbm),
        (shape((exps * heads, rows, rows), low), hbm),
        (shape((exps, rows, head_cols), low), hbm),
        (shape((exps, rows, width), low), hbm),
        (shape((exps, 3 * head_cols, row_block), low), hbm),
        (shape((exps, reps, row_block, out_cols), low), hbm),
        (shape((rows, width), full), vmem),
        (shape((rows, width), low), vmem),
        (shape((rows, 128), full), vmem),
        (shape(expert_in.shape, low), hbm),
        (shape(expert_out.shape, low), hbm),
    ]
    dma = pltpu.SemaphoreType.DMA
    chips = members // 2
    return pl.pallas_call(
        functools.partial(forward_kernel, grps, exps),
        out_shape=[r[0] for r in results],
        in_specs=[smem] * 2 + [vmem] * 7 + [hbm] * 2,
        out_specs=[r[1] for r in results],
        scratch_shapes=[
            pltpu.VMEM(expert_in.shape, full),
            pltpu.VMEM(expert_out.shape, full),
            pltpu.VMEM((shard_cols, row_block), low),
            pltpu.VMEM((row_block, out_cols), low),
            pltpu.VMEM(expert_in.shape, low),
            pltpu.VMEM(expert_out.shape, low),
            pltpu.VMEM((exps, rows, width), low),
            pltpu.VMEM((exps, 3 * head_cols, row_block), low),
            pltpu.VMEM((exps, reps, row_block, out_cols), low),
            pltpu.VMEM((exps, rows, width), low),
            pltpu.VMEM((exps, rows, 3 * head_cols), low),
            pltpu.VMEM((exps * heads, rows, rows), low),
            pltpu.VMEM((exps, rows, head_cols), low),
            pltpu.VMEM((exps, rows, head_cols), low),
            pltpu.VMEM((heads, rows, rows), full),
            pltpu.VMEM((8, rows), full),
            pltpu.VMEM((tiles.skip, width), low),
            dma((2, exps)),
            dma((2, max(segs * (QUAD + grps - 1), exps * 3 * head_cols // seg))),
            dma((exps * 3 * head_cols // seg, QUAD - 1)),
            dma((2, reps)),
            dma((2, exps)),
            dma((2, 2, 2 * reps)),
            dma((2, 2, reps + 1)),
            dma((2, exps)),
            dma((2, 3 * chips)),
            dma((2, 3 * chips + 1)),
            dma((2, 3 * chips)),
            dma((2, 3 * chips + 1)),
            dma((2, members)),
            dma((8,)),
            dma((2,)),
        ],
        compiler_params=pltpu.CompilerParams(
            collective_id=0, has_side_effects=True, vmem_limit_bytes=60 * 1024 * 1024
        ),
        name="forward",
    )(lengths, bias_table, routes_t, tokens, cotangent, gains, router, attn_qkv, attn_out, expert_in, expert_out)


def expert_kernel(
    grps,
    exps,
    cap,
    deal,
    routes_t,
    comb,
    n_all,
    cot_all,
    both_w,
    down_w,
    in_low,
    down_slab,
    h1,
    n_total,
    y_half,
    y_far,
    c_in,
    both_g,
    down_g,
    in_parts,
    down_parts,
    place,
    marks,
    n_rows,
    g_rows,
    both_v,
    down_v,
    raw_n,
    raw_g,
    y_acc,
    n_acc,
    both_d,
    active,
    n_bufs,
    c_sum,
    out_y,
    load_sem,
    raw_sem,
    out_sem,
    in_sem,
    in_down_sem,
    home_sem,
    home_down_sem,
    stage_sem,
    far_sem,
    n_sem,
    c_sem,
):
    at = Where(grps, exps)
    rows, width = n_all.shape[1:]
    tiles = Tiles(down_slab.shape[0], at.reps)
    size = tiles.size
    slots = exps * cap
    members = QUAD * exps
    loads = [pltpu.make_async_copy(both_w.at[t], both_v.at[t], load_sem.at[0, t]) for t in range(2)] + [
        pltpu.make_async_copy(down_w.at[t], down_v.at[t], load_sem.at[1, t]) for t in range(2)
    ]
    for copy in loads:
        copy.start()

    def raw_copies(q):
        here = pl.ds(pl.multiple_of(q * exps, exps), exps)
        return [
            pltpu.make_async_copy(n_all.at[here], raw_n.at[pl.ds(q % 2 * exps, exps)], raw_sem.at[0, q % 2]),
            pltpu.make_async_copy(cot_all.at[here], raw_g.at[pl.ds(q % 2 * exps, exps)], raw_sem.at[1, q % 2]),
        ]

    for copy in raw_copies(0):
        copy.start()

    beside = at.exp + 1 - 2 * (at.exp % 2)
    greet(*neighbours(at))()
    last = tiles.count - 1
    incoming = Outward(
        at, tiles, last, in_low, down_slab, both_v.at[last], down_v.at[last], None, in_sem, in_down_sem
    )
    incoming.start()
    home = Homeward(
        at, tiles, 0, both_v.at[0], down_v.at[0], in_parts, down_parts, home_sem, home_down_sem, (0,)
    )

    earlier = jnp.where(row_of((rows, rows)) < lane_of((rows, rows)), 1.0, 0.0).astype(low)
    slot = row_of((cap, rows)).astype(full)

    def dispatch(q, _):
        @pl.when(q + 1 < QUAD)
        def _():
            for copy in raw_copies(q + 1):
                copy.start()

        for copy in raw_copies(q):
            copy.wait()
        lines = []
        for j in range(exps):
            seq = at.grp * members + q * exps + j
            pair = routes_t[:, pl.ds(pl.multiple_of(seq * rows, rows), rows)]
            lines.append(jnp.logical_or(pair[0:1] == at.exp, pair[1:2] == at.exp))
        lines = [jnp.where(line, 1.0, 0.0) for line in lines] + [jnp.zeros((8 - exps, rows), full)]
        hot_low = jnp.concatenate(lines, axis=0).astype(low)
        before = dot(hot_low, earlier)
        for j in range(exps):
            s = q * exps + j
            inside = jnp.logical_and(slot == before[j : j + 1, :], hot_low[j : j + 1, :].astype(full) > 0.5)
            here = jnp.where(inside, 1.0, 0.0)
            place[s] = here.astype(low)
            g = raw_g[q % 2 * exps]
            for b in range(1, exps):
                g = jnp.where(deal[at.grp * members + s] == at.grp * members + q * exps + b, raw_g[q % 2 * exps + b], g)
            where = pl.ds(pl.multiple_of(s * cap, cap), cap)
            n_rows[where] = dot(here.astype(low), raw_n[q % 2 * exps + j]).astype(low)
            g_rows[where] = dot(here.astype(low), g).astype(low)
            marks[where, 0:1] = jnp.sum(here * comb[s, pl.ds(at.exp, 1), :], axis=1, keepdims=True)
            marks[where, 1:2] = jnp.zeros((cap, 1), full)
        return 0

    lax.fori_loop(0, QUAD, dispatch, 0)
    for copy in loads:
        copy.wait()
    curve = math.sqrt(2.0 / math.pi)

    core = at.exp % 2

    plane = at.quad * exps + at.exp
    sibling = at.device(at.rep, beside)
    dn = Halving(at, n_bufs, n_sem, [[0, 1, 2], [1, 2, 0], [2, 0, 1]])

    def n_copy(j):
        return send(raw_n.at[j], n_bufs[0].at[j], far_sem.at[0, 0, j], far_sem.at[0, 1, j], sibling)

    def y_copies(j):
        return (
            pltpu.make_async_copy(out_y.at[j % 2], y_half.at[j], out_sem.at[j % 2]),
            send(raw_n.at[j], y_far.at[j], far_sem.at[1, 0, j], far_sem.at[1, 1, j], sibling),
        )

    def c_copy(k):
        other = (plane + k) % members
        return send(
            c_sum.at[other],
            c_in.at[plane],
            c_sem.at[0, other],
            c_sem.at[1, plane],
            (at.grp, other // exps, other % exps),
        )

    def slots_of(s):
        return pl.ds(pl.multiple_of(s * cap, cap), cap)

    def n_rows_of(s):
        where = slots_of(s)
        line = jnp.sum(place[s].astype(full) * marks[where, 1:2], axis=0, keepdims=True)
        c_sum[s] = jnp.broadcast_to(line, (8, rows))
        return tn(place[s], n_acc[where]).astype(low)

    def y_rows_of(p):
        first = p // exps * exps
        spot = at.grp * members + p
        here, y = place[first], y_acc[slots_of(first)]
        for c in range(1, exps):
            taken = deal[at.grp * members + first + c] == spot
            here = jnp.where(taken, place[first + c], here)
            y = jnp.where(taken, y_acc[slots_of(first + c)], y)
        return (tn(here, y) + jnp.where(deal[at.me] == spot, h1[...], 0.0)).astype(low)

    def give_n(j):
        raw_n[j] = n_rows_of(2 * j + 1 - core)
        n_copy(j).start()
        raw_g[j] = n_rows_of(2 * j + core)

    def add_n(quad):
        for k in range(exps // 2):
            j = quad * (exps // 2) + k
            arrived(n_bufs[0].at[j], far_sem.at[0, 1, j])
            n_bufs[0][j] = n_bufs[0][j] + raw_g[j]

    def give_y(j, _):
        @pl.when(j >= 2)
        def _():
            y_copies(j - 2)[0].wait()

        out_y[j % 2] = y_rows_of(2 * j + core)
        n_copy(j).wait_send()
        raw_n[j] = y_rows_of(2 * j + 1 - core)
        for copy in y_copies(j):
            copy.start()
        return 0

    def start_c(k, _):
        c_copy(k).start()
        return 0

    def tile_work(f, _):
        @pl.when(f == last)
        def _():
            incoming.arrive()

        def chunk(i, _):
            c = jnp.where(i == 0, at.near(3), jnp.where(i == 1, at.near(1), jnp.where(i == 2, at.near(2), at.quad)))
            here = pl.ds(pl.multiple_of(c * slots, slots), slots)
            share = marks[here, 0:1]
            both = dot(n_rows[here], both_v[f])
            gate_part, up_part = both[:, :size], both[:, size:]
            grad = nt(g_rows[here], down_v[f])
            square = gate_part * gate_part
            bend = jnp.tanh(curve * gate_part * (1.0 + 0.044715 * square))
            half = 0.5 * (1.0 + bend)
            gelu = gate_part * half
            slope = half + (0.5 * curve) * gate_part * (1.0 - bend * bend) * (1.0 + (3 * 0.044715) * square)
            value = gelu * up_part
            marks[here, 1:2] += jnp.sum(value * grad, axis=1, keepdims=True)
            grad = grad * share
            active[f % 2, here] = (value * share).astype(low)
            both_d[f % 2, here, :size] = (grad * up_part * slope).astype(low)
            both_d[f % 2, here, size:] = (grad * gelu).astype(low)
            y = dot(active[f % 2, here], down_v[f])
            y_acc[here] = jnp.where(f == 0, y, y_acc[here].astype(full) + y).astype(low)
            n_back = nt(both_d[f % 2, here], both_v[f])
            n_acc[here] = jnp.where(f == 0, n_back, n_acc[here].astype(full) + n_back).astype(low)

            @pl.when(f == last)
            def _():
                for k in range(exps // 2):
                    give_n(c * (exps // 2) + k)

            @pl.when(jnp.logical_and(f == last, i == 2))
            def _():
                add_n(at.near(3))

            @pl.when(jnp.logical_and(f == last, i == 3))
            def _():
                add_n(at.near(1))
                dn.start(0, 1)

            return 0

        lax.fori_loop(0, QUAD, chunk, 0)

        @pl.when(f == 0)
        def _():
            weight_work(0)

        return 0

    def weight_work(f):
        def columns(m, _):
            cols = pl.ds(pl.multiple_of(m * (width // 2), width // 2), width // 2)
            both_v[f, cols] = tn(n_rows[:, cols], both_d[f % 2]).astype(low)
            down_v[f, :, cols] = tn(active[f % 2], g_rows[:, cols]).astype(low)
            return 0

        lax.fori_loop(0, 2, columns, 0)

        for copy in stage_copies(f):
            copy.start()
        if f == 0:
            home.start()

    def stage_copies(f):
        copies = [pltpu.make_async_copy(both_v.at[f], both_g.at[f], stage_sem.at[0, f])]
        if f:
            copies.append(pltpu.make_async_copy(down_v.at[f], down_g.at[f - 1], stage_sem.at[1, f]))
        return copies

    lax.fori_loop(0, tiles.count, tile_work, 0)

    half = members // 2
    lax.fori_loop(1, members, start_c, 0)
    c_in[plane] = c_sum[plane]
    weight_work(1)
    add_n(at.near(2))
    dn.start(0, 2)
    add_n(at.quad)
    dn.start(0, 0)
    weight_work(2)
    lax.fori_loop(0, half, give_y, 0)
    for step in range(len(dn.chip_bits)):
        dn.next(step)
    n_total[...] = dn.result()[0]
    for j in (half - 2, half - 1):
        y_copies(j)[0].wait()
    for f in range(tiles.count):
        for copy in stage_copies(f):
            copy.wait()

    def core_in(j, _):
        y_copies(j)[1].wait_send()
        arrived(y_far.at[j], far_sem.at[1, 1, j])
        return 0

    lax.fori_loop(0, half, core_in, 0)

    def c_done(k, _):
        c_copy(k).wait_send()
        other = (plane + k) % members
        arrived(c_in.at[other], c_sem.at[1, other])
        return 0

    lax.fori_loop(1, members, c_done, 0)
    dn.finish()
    home.arrive()
    incoming.sent()
    home.sent()


def expert_call(grps, exps, cap, deal, routes_t, comb_all, n_all, cot_all, both_w, down_w, in_low, down_slab, h1):
    members, rows, width = n_all.shape
    reps = grps * QUAD
    tiles = Tiles(down_slab.shape[0], reps)
    size = tiles.size
    slab, both_hidden = in_low.shape
    units = down_slab.shape[0]
    slots = exps * cap
    chip_bits = bits_of(members) - 1
    shape = jax.ShapeDtypeStruct
    vmem = pl.BlockSpec(memory_space=pltpu.VMEM)
    smem = pl.BlockSpec(memory_space=pltpu.SMEM)
    hbm = pl.BlockSpec(memory_space=pl.ANY)
    results = [
        (shape((rows, width), low), vmem),
        (shape((members // 2, rows, width), low), hbm),
        (shape((members // 2, rows, width), low), hbm),
        (shape((members, 8, rows), full), vmem),
        (shape((tiles.count, width, 2 * size), low), hbm),
        (shape((2, size, width), low), hbm),
        (shape((grps, slab, both_hidden), low), hbm),
        (shape((grps, units, width), low), hbm),
    ]
    dma = pltpu.SemaphoreType.DMA
    return pl.pallas_call(
        functools.partial(expert_kernel, grps, exps, cap),
        out_shape=[r[0] for r in results],
        in_specs=[smem] + [vmem] * 2 + [hbm] * 6 + [vmem],
        out_specs=[r[1] for r in results],
        scratch_shapes=[
            pltpu.VMEM((members, cap, rows), low),
            pltpu.VMEM((QUAD * slots, 128), full),
            pltpu.VMEM((QUAD * slots, width), low),
            pltpu.VMEM((QUAD * slots, width), low),
            pltpu.VMEM((tiles.count, width, 2 * size), low),
            pltpu.VMEM((tiles.count, size, width), low),
            pltpu.VMEM((2 * exps, rows, width), low),
            pltpu.VMEM((2 * exps, rows, width), low),
            pltpu.VMEM((QUAD * slots, width), low),
            pltpu.VMEM((QUAD * slots, width), low),
            pltpu.VMEM((2, QUAD * slots, 2 * size), low),
            pltpu.VMEM((2, QUAD * slots, size), low),
            [pltpu.VMEM((members >> (1 + step), rows, width), low) for step in range(chip_bits + 1)],
            pltpu.VMEM((members, 8, rows), full),
            pltpu.VMEM((2, rows, width), low),
            dma((2, 2)),
            dma((2, 2)),
            dma((2,)),
            dma((2, 2 * reps)),
            dma((2, reps + 1)),
            dma((2, 2 * reps)),
            dma((2, max(QUAD, grps))),
            dma((2, tiles.count)),
            dma((2, 2, members // 2)),
            dma((2, 3 << chip_bits)),
            dma((2, members)),
        ],
        compiler_params=pltpu.CompilerParams(
            collective_id=2, has_side_effects=True, vmem_limit_bytes=60 * 1024 * 1024
        ),
        name="experts",
    )(deal, routes_t, comb_all, n_all, cot_all, both_w, down_w, in_low, down_slab, h1)


def adamw_root(weight, moment, second, gradient, step_rate, decay_factor):
    new_moment = beta_one * moment + (1.0 - beta_one) * gradient
    new_second = beta_two * second + (1.0 - beta_two) * gradient * gradient
    root = lax.rsqrt(new_second * (1.0 / (1.0 - beta_two**STEP)))
    step = new_moment * (root * (1.0 - eps_adam * root))
    keep = 1.0 - step_rate * decay_factor
    return (new_moment, new_second, keep * weight - (step_rate / (1.0 - beta_one**STEP)) * step)


def adam_kernel(exps, *refs):
    in_parts, down_parts, qkv_grad, out_grad, small = refs[:5]
    states, news, bias_grad = refs[5:26], refs[26:47], refs[47]
    heads = HEADS // exps
    width = small.shape[1]

    def update(i, grad, rate, decay):
        weight, first, second = [state[...] for state in states[3 * i : 3 * i + 3]]
        values = adamw_root(weight, first, second, grad, rate, decay)
        for new, value in zip(news[3 * i : 3 * i + 3], values, strict=True):
            new[...] = value

    def total(parts):
        result = parts[0].astype(full)
        for k in range(1, parts.shape[0]):
            result = result + parts[k].astype(full)
        return result

    @pl.when(pl.program_id(0) == 0)
    def _():
        update(0, qkv_grad[...], 1.5 / math.sqrt(D), 0.1)
        update(1, out_grad[...], 6.0 / math.sqrt(D), 0.1)
        for e in range(exps):
            for h in range(heads):
                bias_grad[e * heads + h : e * heads + h + 1, :] = small[
                    exps + 3 + e : exps + 4 + e, h * 128 : h * 128 + BUCKETS
                ]
        update(2, bias_grad[...], 0.3, 0.0)
        update(3, small[0:exps, :], 1.0 / math.sqrt(D), 0.1)
        update(4, small[exps : exps + 2, :], 0.5, 0.0)

    update(5, total(in_parts), 1.5 / math.sqrt(D), 0.1)
    update(6, total(down_parts), 1.5 / math.sqrt(FF), 0.1)


def adam_call(exps, in_parts, down_parts, qkv_grad, out_grad, small, states):
    steps = 4

    def whole(array):
        return pl.BlockSpec(array.shape, lambda i: (0,) * array.ndim)

    def columns(array):
        block = array.shape[:-1] + (array.shape[-1] // steps,)
        return pl.BlockSpec(block, lambda i: (0,) * (array.ndim - 1) + (i,))

    specs = [whole(state) for state in states[:15]]
    specs += [columns(state) for state in states[15:18]] + [columns(state) for state in states[18:]]
    return pl.pallas_call(
        functools.partial(adam_kernel, exps),
        grid=(steps,),
        in_specs=[columns(in_parts), columns(down_parts), whole(qkv_grad), whole(out_grad), whole(small)] + specs,
        out_specs=specs,
        out_shape=[jax.ShapeDtypeStruct(state.shape, full) for state in states],
        scratch_shapes=[pltpu.VMEM((HEADS, BUCKETS), full)],
        compiler_params=pltpu.CompilerParams(vmem_limit_bytes=60 * 1024 * 1024),
        name="adam",
    )(in_parts, down_parts, qkv_grad, out_grad, small, *states)


def backward_kernel(
    grps,
    exps,
    lengths,
    deal,
    y_half,
    y_far,
    both_g,
    down_g,
    in_before,
    down_before,
    n1_in,
    cot_all,
    routes_t,
    tokens,
    n_total,
    c_in,
    n2_in,
    probs_in,
    h1_from,
    qkv_from,
    pb_from,
    mine_from,
    wqkv_from,
    wout_from,
    gains,
    router_t,
    *rest,
):
    token_grad, block_out, in_parts, down_parts, qkv_grad, out_grad, small_out = rest[:7]
    scratch = rest[7:]
    (
    h1_in,
    qkv,
    pb,
    mine,
    wqkv,
    wout,
    kept,
    y_bufs,
    dh1,
    dz_send,
    dz_all,
    do_send,
    do_in,
    bias_sum,
    dqkv,
    dqkv_t,
    dn1_send,
    dn1_in,
    wq_send,
    og_send,
    mids,
    far_send,
    far_in,
    small_send,
    small_exp,
    small_sum,
    small_rep,
    y_sem,
    load_sem,
    weight_sem,
    down_sem,
    dz_sem,
    do_sem,
    dn1_sem,
    wq_sem,
    og_sem,
    mid_sem,
    far_sem,
    small_sem,
    small2_sem,
    n1_sem,
    operand_sem,
    ) = scratch
    at = Where(grps, exps)
    reps = at.reps
    rows, width = tokens.shape
    heads = HEADS // exps
    head_dim = width // HEADS
    head_cols = heads * head_dim
    block_cols = min(128, head_cols)
    row_block = wqkv.shape[2]
    out_cols = wout.shape[3]
    tiles = Tiles(down_parts.shape[1], reps)
    scale = 1.0 / math.sqrt(head_dim)
    SEND, RECV = 0, 1
    plane = at.quad * exps + at.exp
    members = QUAD * exps

    def exp_peer(k):
        return (at.exp + k) % exps

    router = router_t[...]
    met = greet(*neighbours(at))
    n1 = kept.at[0:exps]
    group = pl.ds(pl.multiple_of(at.quad * exps, exps), exps)
    cot_copy = pltpu.make_async_copy(cot_all.at[group], dn1_send, n1_sem.at[1])
    cot_copy.start()
    loads = [
        pltpu.make_async_copy(src, dst, operand_sem.at[i])
        for i, (src, dst) in enumerate(
            ((h1_from, h1_in), (wout_from, wout), (qkv_from, qkv), (pb_from, pb), (mine_from, mine), (wqkv_from, wqkv))
        )
    ]
    ys = Halving(at, y_bufs, y_sem, [[0, 1, 2], [0, 1, 2], [1, 0, 2]])
    half_loads = [
        pltpu.make_async_copy(y_far, y_bufs[0], load_sem.at[0]),
        pltpu.make_async_copy(y_half, kept, load_sem.at[1]),
    ]
    for copy in loads + half_loads:
        copy.start()

    span = 2 * rows
    met()

    homes = [
        Homeward(
            at,
            tiles,
            t,
            both_g.at[t],
            down_g.at[t - 1] if t else None,
            in_parts,
            down_parts,
            weight_sem.at[t],
            down_sem.at[t],
            (0, 1) if t else (1,),
        )
        for t in range(tiles.count)
    ]
    homes[0].start()
    homes[1].start()
    n1_copy = pltpu.make_async_copy(n1_in, n1, n1_sem.at[0])

    lane = lane_of((rows, 128))
    comb_rows = []
    for e in range(exps):
        total = c_in[e]
        for q in range(1, QUAD):
            total = total + c_in[q * exps + e]
        comb_rows.append(total[0:1, :])
    comb_rows.append(jnp.zeros((128 - exps, rows), full))
    comb_grad = jnp.concatenate(comb_rows, axis=0).T
    valid = row_of((rows, 1)) < lengths[at.me]
    probs = probs_in[...]
    hot = routed(routes_t, at.me, rows)
    picked = jnp.where(hot, probs, 0.0)
    total = jnp.sum(picked, axis=1, keepdims=True)
    gate = picked / total
    gate_grad_rows = jnp.where(valid, comb_grad, 0.0)
    spread_grad = jnp.sum(gate_grad_rows * gate, axis=1, keepdims=True)
    probs_grad = jnp.where(hot, (gate_grad_rows - spread_grad) / total, 0.0)
    logit_grad = probs * (probs_grad - jnp.sum(probs_grad * probs, axis=1, keepdims=True))
    small_rows = small_send.shape[0]
    small_send[...] = jnp.zeros_like(small_send)
    router_back = jnp.dot(
        logit_grad, jnp.concatenate([router, jnp.zeros((128 - exps, width), full)], axis=0),
        precision=highest, preferred_element_type=full,
    )
    for copy in loads:
        copy.wait()
    h1 = h1_in[...]
    r2 = lax.rsqrt(jnp.mean(h1 * h1, axis=1, keepdims=True) + eps_norm)

    steps = len(ys.chip_bits)
    n2_grad = router_back + n_total[...].astype(full)
    scaled = n2_grad * gains[1:2, :]
    cot_copy.wait()
    dealt = deal[at.me] - at.base
    g = dn1_send[0]
    for e in range(1, exps):
        g = jnp.where(dealt == e, dn1_send[e], g)
    hidden_grad = (
        jnp.where(valid, g.astype(full), 0.0)
        + r2 * scaled
        - h1 * (r2 * r2 * r2) * jnp.mean(scaled * h1, axis=1, keepdims=True)
    )
    dh1[...] = hidden_grad
    small_send[exps + 1 : exps + 2, :] = jnp.sum(n2_grad * h1 * r2, axis=0, keepdims=True)
    branch = hidden_grad.astype(low)
    dz_send[...] = branch
    for e in range(exps):
        total = jnp.zeros((rows, row_block), full)
        for r in range(reps):
            total = total + nt(branch[:, r * out_cols : (r + 1) * out_cols], wout[e, r])
        do_send[e] = total.astype(low)

    def do_copies():
        return [
            send(
                do_send.at[exp_peer(k)],
                do_in.at[at.exp],
                do_sem.at[SEND, exp_peer(k)],
                do_sem.at[RECV, at.exp],
                at.device(at.rep, exp_peer(k)),
            )
            for k in range(1, exps)
        ]

    for copy in do_copies():
        copy.start()
    pltpu.make_async_copy(do_send.at[at.exp], do_in.at[at.exp], do_sem.at[RECV, at.exp]).start()

    group_dz = Group(at, dz_send, dz_all, dz_sem)
    group_dz.start()
    dz_all[at.exp] = branch
    for copy in half_loads:
        copy.wait()

    def add_halves(j, _):
        y_bufs[0][j] = y_bufs[0][j] + kept[j]
        return 0

    lax.fori_loop(0, kept.shape[0], add_halves, 0)
    ys.start(0)
    n1_copy.start()

    bias_sum[...] = jnp.zeros_like(bias_sum)

    def dn1_copies():
        beside, across = turn(at.exp, 2), turn(at.exp, 1)
        return [
            functools.partial(
                send, dn1_send.at[k], dn1_in.at[j], dn1_sem.at[SEND, j], dn1_sem.at[RECV, j], at.device(at.rep, to)
            )
            for k, j, to in ((turn(at.exp, 0), 2, beside), (across, 0, across), (beside, 1, beside))
        ]

    def attend_back(i, _):
        s = turn(at.exp, i)
        @pl.when(i == 1)
        def _():
            group_dz.pass_on()

        arrived(do_in.at[s], do_sem.at[RECV, s])
        block_lane = lane_of((rows, block_cols))
        for c in range(head_cols // block_cols):
            cols = slice(c * block_cols, (c + 1) * block_cols)
            k_cols = slice(head_cols + c * block_cols, head_cols + (c + 1) * block_cols)
            v_cols = slice(2 * head_cols + c * block_cols, 2 * head_cols + (c + 1) * block_cols)
            q = qkv[s, :, cols] * scale
            k = qkv[s, :, k_cols]
            v = qkv[s, :, v_cols]
            do = do_in[s, :, cols]
            dq = jnp.zeros((rows, block_cols), full)
            dk = jnp.zeros((rows, block_cols), full)
            dv = jnp.zeros((rows, block_cols), full)
            for t in range(block_cols // head_dim):
                h = c * (block_cols // head_dim) + t
                here = jnp.logical_and(block_lane >= t * head_dim, block_lane < (t + 1) * head_dim)
                zero = jnp.zeros_like(q)
                do_h = jnp.where(here, do, zero)
                weights = pb[s * heads + h]
                p = weights.astype(full)
                dp = nt(do_h, v)
                delta = jnp.sum(dp * p, axis=1, keepdims=True)
                ds = (p * (dp - delta)).astype(low)
                bias_sum[h] += ds.astype(full)
                dv = jnp.where(here, tn(weights, do), dv)
                dq = jnp.where(here, jnp.dot(ds, k, preferred_element_type=full), dq)
                dk = jnp.where(here, tn(ds, q), dk)
            dqkv[:, cols] = (dq * scale).astype(low)
            dqkv[:, k_cols] = dk.astype(low)
            dqkv[:, v_cols] = dv.astype(low)
        dqkv_t[:, pl.ds(pl.multiple_of(s * rows, rows), rows)] = dqkv[...].T
        for e in range(exps):
            dn1_send[s, :, e * row_block : (e + 1) * row_block] = jnp.dot(
                dqkv[...], wqkv[e], preferred_element_type=full
            ).astype(low)

        @pl.when(i == 0)
        def _():
            dn1_copies()[0]().start()

        @pl.when(i == 1)
        def _():
            arrived(dn1_in.at[2], dn1_sem.at[RECV, 2])
            dn1_send[s] = (dn1_send[s].astype(full) + dn1_in[2].astype(full)).astype(low)
            dn1_copies()[1]().start()

        @pl.when(i == 2)
        def _():
            dn1_copies()[2]().start()

        return 0

    lax.fori_loop(0, exps, attend_back, 0)

    n1_copy.wait()
    seg = wq_send.shape[2]
    parts = wq_send.shape[1]
    segs = mids.shape[1] - 1
    for e in range(exps):
        part = kept[0:exps, :, e * row_block : (e + 1) * row_block].reshape(exps * rows, row_block)
        total = dot(dqkv_t[...], part)
        for j in range(parts):
            wq_send[e, j] = total[j * seg : (j + 1) * seg].astype(low)

    def owner(j):
        section, within = j // (head_cols // seg), j % (head_cols // seg)
        col = section * width + at.exp * head_cols + within * seg
        block = col // seg
        return block // segs, block % segs

    def mid_place(grp, k, quad):
        return (grp * (segs + 1) + k) * QUAD + quad

    def mid_copy(src, send_sem, rep, k, e):
        dst = mids.at[rep // QUAD, k, at.quad]
        recv = mid_sem.at[mid_place(rep // QUAD, k, at.quad)]
        stays = jnp.logical_and(rep % QUAD == at.quad, e == at.exp)
        return (
            stays,
            functools.partial(send, src, dst, send_sem, recv, (at.grp, rep % QUAD, e)),
            functools.partial(pltpu.make_async_copy, src, dst, recv),
        )

    def wq_copy(i):
        e, j = i // parts, i % parts
        rep, k = owner(j)
        return mid_copy(wq_send.at[e, j], wq_sem.at[i], rep, k, e)

    def og_copy(r):
        return mid_copy(og_send.at[r], og_sem.at[r], r, segs, at.exp)

    def go(copies, act, act_local):
        stays, away, local = copies

        @pl.when(jnp.logical_not(stays))
        def _():
            act(away)

        if act_local:

            @pl.when(stays)
            def _():
                act_local(local)

    def over(count, copies, act, act_local):
        def one(i, _):
            go(copies(i), act, act_local)
            return 0

        lax.fori_loop(0, count, one, 0)

    over(exps * parts, wq_copy, lambda copy: copy().start(), lambda copy: copy().start())
    group_dz.arrive()
    grad = tn(mine[...].reshape(exps * rows, head_cols), dz_all[...].reshape(exps * rows, width))
    for r in range(reps):
        og_send[r] = grad[:, r * out_cols : (r + 1) * out_cols].T.astype(low)
    over(reps, og_copy, lambda copy: copy().start(), lambda copy: copy().start())
    homes[2].start()

    n1_grad = dn1_send[at.exp].astype(full)
    for j in range(2):
        arrived(dn1_in.at[j], dn1_sem.at[RECV, j])
        n1_grad = n1_grad + dn1_in[j].astype(full)
    x = tokens[...].astype(full)
    r1 = lax.rsqrt(jnp.mean(x * x, axis=1, keepdims=True) + eps_norm)
    scaled = n1_grad * gains[0:1, :]
    token_grad[...] = (
        dh1[...] + r1 * scaled - x * (r1 * r1 * r1) * jnp.mean(scaled * x, axis=1, keepdims=True)
    )
    small_send[exps : exps + 1, :] = jnp.sum(n1_grad * x * r1, axis=0, keepdims=True)

    router_rows = lax.dot_general(
        logit_grad, n2_in[...].astype(full), (((0,), (0,)), ((), ())), preferred_element_type=full, precision=highest
    )
    small_send[0:exps, :] = router_rows[0:exps, :]

    line_lane = lane_of((8, 128))
    line_row = row_of((8, 128))
    bias_line = jnp.zeros((8, 128), full)
    flip = jnp.where(row_of((rows, rows)) + lane_of((rows, rows)) == rows - 1, 1.0, 0.0).astype(low)
    turned_bucket = bucket_of(rows - 1 - lane_of((8, span)))
    for h in range(heads):
        high = bias_sum[h].astype(low)
        rest = (bias_sum[h] - high.astype(full)).astype(low)
        flipped = dot(high, flip) + dot(rest, flip)
        square = jnp.concatenate([flipped, jnp.zeros((rows, rows), full)], axis=1)
        turned = pltpu.roll(square, 0, 1, stride=1, stride_axis=0)
        sums = jnp.broadcast_to(jnp.sum(turned, axis=0, keepdims=True), (8, span))
        for b in range(BUCKETS):
            value = jnp.sum(jnp.where(turned_bucket == b, sums, 0.0), axis=1, keepdims=True)
            bias_line = jnp.where(jnp.logical_and(line_row == h, line_lane == b), value, bias_line)
    for h in range(heads):
        small_send[exps + 2 : exps + 3, h * 128 : (h + 1) * 128] = bias_line[h : h + 1, :]

    def small_copies():
        return [
            send(
                small_send,
                small_exp.at[at.exp],
                small_sem.at[SEND, exp_peer(k)],
                small_sem.at[RECV, at.exp],
                at.device(at.rep, exp_peer(k)),
            )
            for k in range(1, exps)
        ]

    for copy in small_copies():
        copy.start()
    small_exp[at.exp] = small_send[...]
    ys.next(0)

    def mid_sum(grp, k):
        for q in range(QUAD):
            arrived(mids.at[grp, k, q], mid_sem.at[mid_place(grp, k, q)])
        total = mids[grp, k, 0].astype(full)
        for q in range(1, QUAD):
            total = total + mids[grp, k, q].astype(full)
        return total

    far = 1 - at.grp
    for k in range(segs + 1):
        far_send[k] = mid_sum(far, k).astype(low)

    def far_copy():
        return send(far_send, far_in, far_sem.at[SEND], far_sem.at[RECV], (far, at.quad, at.exp))

    far_copy().start()
    ys.next(1)
    for k in range(1, exps):
        arrived(small_exp.at[exp_peer(k)], small_sem.at[RECV, exp_peer(k)])
    total = small_exp[0]
    for e in range(1, exps):
        total = total + small_exp[e]
    small_sum[0] = total
    for e in range(exps):
        small_sum[0, exps + 3 + e : exps + 4 + e, :] = small_exp[e, exps + 2 : exps + 3, :]

    def small2_copies():
        return [
            send(
                small_sum.at[0],
                small_rep.at[at.rep],
                small2_sem.at[SEND, (at.rep + k) % reps],
                small2_sem.at[RECV, at.rep],
                at.device((at.rep + k) % reps, at.exp),
            )
            for k in range(1, reps)
        ]

    for copy in small2_copies():
        copy.start()
    small_rep[at.rep] = small_sum[0]
    for step in range(2, steps):
        ys.next(step)
    length = lengths[at.base]
    for e in range(1, exps):
        length = jnp.where(deal[at.base + e] == at.me, lengths[at.base + e], length)
    block = ys.result()[0]
    block_out[...] = jnp.where(row_of((rows, 1)) < length, block, jnp.zeros_like(block))
    for k in range(1, reps):
        arrived(small_rep.at[(at.rep + k) % reps], small2_sem.at[RECV, (at.rep + k) % reps])
    total = small_rep[0]
    for r in range(1, reps):
        total = total + small_rep[r]
    small_out[...] = total

    near = [mid_sum(at.grp, k) for k in range(segs + 1)]
    arrived(far_in, far_sem.at[RECV])
    grads = [(near[k] + far_in[k].astype(full)).T for k in range(segs + 1)]
    qkv_grad[...] = jnp.concatenate(grads[:segs], axis=1)
    out_grad[...] = grads[segs]
    for home in homes:
        home.arrive()

    ys.finish()

    for home in homes:
        home.sent()

    over(exps * parts, wq_copy, lambda copy: copy().wait_send(), None)
    over(reps, og_copy, lambda copy: copy().wait_send(), None)
    far_copy().wait_send()
    for copies in (do_copies(), small_copies(), small2_copies()):
        for copy in copies:
            copy.wait_send()
    for copy in dn1_copies():
        copy().wait_send()
    group_dz.sent()


def routed(routes_t, seq, rows):
    pair = routes_t[:, pl.ds(pl.multiple_of(seq * rows, rows), rows)].astype(full)
    cols = jnp.concatenate([pair, jnp.zeros((126, rows), full)], axis=0).T
    lane = lane_of((rows, 128)).astype(full)
    return jnp.logical_or(lane == cols[:, 0:1], lane == cols[:, 1:2])


def backward_call(
    grps, exps, lengths, deal, y_half, y_far, both_g, down_g, in_before, down_before, n1,
    cot_all, routes_t, tokens, n_total, c_in, n2, probs, h1, qkv, pb, mine, wqkv, wout, gains, router
):
    reps = grps * QUAD
    rows, width = tokens.shape
    heads = HEADS // exps
    head_cols = width // exps
    row_block = wqkv.shape[2]
    out_cols = wout.shape[3]
    shard_cols = 3 * width // reps
    seg = math.gcd(shard_cols, head_cols)
    segs = shard_cols // seg
    parts = 3 * head_cols // seg
    members = QUAD * exps
    chip_bits = bits_of(members) - 1
    small_rows = -(-(2 * exps + 3) // 8) * 8
    shape = jax.ShapeDtypeStruct
    vmem = pl.BlockSpec(memory_space=pltpu.VMEM)
    smem = pl.BlockSpec(memory_space=pltpu.SMEM)
    hbm = pl.BlockSpec(memory_space=pl.ANY)
    results = [
        (shape((rows, width), full), vmem),
        (shape((rows, width), low), vmem),
        (shape(in_before.shape, low), hbm),
        (shape(down_before.shape, low), hbm),
        (shape((row_block, shard_cols), full), vmem),
        (shape((row_block, out_cols), full), vmem),
        (shape((small_rows, width), full), vmem),
    ]
    dma = pltpu.SemaphoreType.DMA
    bufs = [pltpu.VMEM((1 << (chip_bits - s), rows, width), low) for s in range(chip_bits + 1)]
    return pl.pallas_call(
        functools.partial(backward_kernel, grps, exps),
        out_shape=[r[0] for r in results],
        in_specs=[smem] * 2 + [hbm] * 8 + [vmem] * 6 + [hbm] * 6 + [vmem] * 2,
        out_specs=[r[1] for r in results],
        scratch_shapes=[
            pltpu.VMEM(h1.shape, full),
            pltpu.VMEM(qkv.shape, low),
            pltpu.VMEM(pb.shape, low),
            pltpu.VMEM(mine.shape, low),
            pltpu.VMEM(wqkv.shape, low),
            pltpu.VMEM(wout.shape, low),
            pltpu.VMEM((members // 2, rows, width), low),
            list(bufs),
            pltpu.VMEM((rows, width), full),
            pltpu.VMEM((rows, width), low),
            pltpu.VMEM((exps, rows, width), low),
            pltpu.VMEM((exps, rows, head_cols), low),
            pltpu.VMEM((exps, rows, head_cols), low),
            pltpu.VMEM((heads, rows, rows), full),
            pltpu.VMEM((rows, 3 * head_cols), low),
            pltpu.VMEM((3 * head_cols, exps * rows), low),
            pltpu.VMEM((exps, rows, width), low),
            pltpu.VMEM((3, rows, width), low),
            pltpu.VMEM((exps, parts, seg, row_block), low),
            pltpu.VMEM((reps, seg, row_block), low),
            pltpu.VMEM((grps, segs + 1, QUAD, seg, row_block), low),
            pltpu.VMEM((segs + 1, seg, row_block), low),
            pltpu.VMEM((segs + 1, seg, row_block), low),
            pltpu.VMEM((small_rows, width), full),
            pltpu.VMEM((exps, small_rows, width), full),
            pltpu.VMEM((1, small_rows, width), full),
            pltpu.VMEM((reps, small_rows, width), full),
            dma((2, 3 << chip_bits)),
            dma((2,)),
            dma((3, 2, 2 * reps)),
            dma((3, 2, max(QUAD, grps))),
            dma((2, exps)),
            dma((2, exps)),
            dma((2, exps)),
            dma((exps * parts,)),
            dma((reps,)),
            dma((grps * (segs + 1) * QUAD,)),
            dma((2,)),
            dma((2, exps)),
            dma((2, reps)),
            dma((2,)),
            dma((6,)),
        ],
        compiler_params=pltpu.CompilerParams(
            collective_id=1, has_side_effects=True, vmem_limit_bytes=60 * 1024 * 1024
        ),
        input_output_aliases={6: 2, 7: 3},
        name="backward",
    )(
        lengths, deal, y_half, y_far, both_g, down_g, in_before, down_before, n1, cot_all,
        routes_t, tokens, n_total, c_in, n2, probs, h1, qkv, pb, mine, wqkv, wout, gains, router
    )


def per_device(
    tokens,
    cotangent,
    seq_lengths,
    deal,
    routes,
    attn_qkv,
    qkv_first,
    qkv_second,
    attn_out,
    out_first,
    out_second,
    rel_bias,
    bias_first,
    bias_second,
    router,
    router_first,
    router_second,
    norm_gains,
    gains_first,
    gains_second,
    expert_in,
    in_first,
    in_second,
    expert_out,
    down_first,
    down_second,
):
    rows, width = tokens.shape
    experts = router.shape[1]
    capacity = (10 * rows + 4 * experts - 1) // (4 * experts)
    exps = lax.axis_size("exp")
    grps = lax.axis_size("grp")
    routes_t = routes.T
    bias_table = rel_bias.T
    (
        both_w, down_w, cot_all, n_all, comb_all, qkv, pb, context_mine, normed_group, wqkv, wout, hidden_one,
        normed_two, router_probs, in_low, down_low,
    ) = forward_call(
        grps, exps, seq_lengths, bias_table, routes_t, tokens, cotangent, norm_gains.T, router.T,
        attn_qkv, attn_out, expert_in[0], expert_out[0],
    )
    n_total, y_half, y_far, c_in, both_g, down_g, in_before, down_before = expert_call(
        grps, exps, capacity, deal, routes_t, comb_all, n_all, cot_all, both_w, down_w, in_low, down_low,
        hidden_one,
    )
    token_grad, block_out, in_parts, down_parts, qkv_grad, out_grad, small = backward_call(
        grps, exps, seq_lengths, deal, y_half, y_far, both_g, down_g,
        in_before, down_before, normed_group, cot_all, routes_t, tokens, n_total, c_in, normed_two, router_probs, hidden_one, qkv, pb, context_mine, wqkv,
        wout, norm_gains.T, router.T,
    )
    states = [
        attn_qkv, qkv_first, qkv_second, attn_out, out_first, out_second, bias_table, bias_first.T, bias_second.T,
        router.T, router_first.T, router_second.T, norm_gains.T, gains_first.T, gains_second.T,
        expert_in[0], in_first[0], in_second[0], expert_out[0], down_first[0], down_second[0],
    ]
    new = list(adam_call(exps, in_parts, down_parts, qkv_grad, out_grad, small, states))
    new = new[:6] + [array.T for array in new[6:15]] + [array[None] for array in new[15:]]
    return (block_out, token_grad, *new)


def bucket_onehot(length):
    places = jnp.arange(length, dtype=jnp.int32)
    offset = places[None, :] - places[:, None]
    distance = jnp.abs(offset)
    bucket = 16 * (offset > 0).astype(jnp.int32)
    for threshold in thresholds:
        bucket = bucket + (distance >= threshold).astype(jnp.int32)
    return (bucket[:, :, None] == jnp.arange(BUCKETS, dtype=jnp.int32)[None, None, :]).astype(full)


def swap(pieces, axes):
    return lax.all_to_all(pieces, axes, split_axis=0, concat_axis=0, tiled=True)


def spread(block, axes):
    members = lax.axis_size(axes)
    return swap(jnp.broadcast_to(block[None], (members,) + block.shape), axes)


def plain_device(
    tokens,
    cotangent,
    seq_lengths,
    deal,
    routes,
    attn_qkv,
    qkv_first,
    qkv_second,
    attn_out,
    out_first,
    out_second,
    rel_bias,
    bias_first,
    bias_second,
    router,
    router_first,
    router_second,
    norm_gains,
    gains_first,
    gains_second,
    expert_in,
    in_first,
    in_second,
    expert_out,
    down_first,
    down_second,
):
    rows, width = tokens.shape
    head_dim = width // HEADS
    score_scale = 1.0 / math.sqrt(head_dim)
    experts = router.shape[1]
    capacity = (10 * rows + 4 * experts - 1) // (4 * experts)
    exps = lax.axis_size("exp")
    grps = lax.axis_size("grp")
    reps = grps * QUAD
    heads = HEADS // exps
    head_cols = heads * head_dim
    place = lax.axis_index("exp")
    base = lax.axis_index(REP) * exps
    me = base + place
    slab = expert_in.shape[1]
    units = expert_out.shape[1]
    quarter = grps * units

    row_block = attn_qkv.shape[0]
    qkv_rows = lax.all_gather(attn_qkv.astype(low), REP, axis=1, tiled=True)
    out_rows = lax.all_gather(attn_out.astype(low), REP, axis=1, tiled=True)
    qkv_pieces = jnp.transpose(
        qkv_rows.reshape(row_block, 3, exps, head_cols), (2, 0, 1, 3)
    ).reshape(exps, row_block, 3 * head_cols)
    qkv_mine = swap(qkv_pieces, "exp").reshape(width, 3 * head_cols)
    full_out = spread(out_rows, "exp").reshape(width, width)

    group_tokens = spread(tokens, "exp")
    group_cotangent = spread(cotangent, "exp")
    my_cotangent = lax.dynamic_index_in_dim(group_cotangent, deal[me] - base, 0, keepdims=False)

    my_routes = lax.dynamic_slice_in_dim(routes, me * rows, rows, 0)
    places = jnp.arange(rows, dtype=jnp.int32)
    valid_rows = (places < seq_lengths[me]).astype(full)
    group_lengths = lax.dynamic_slice_in_dim(seq_lengths, base, exps, 0)
    key_ok = places[None, :] < group_lengths[:, None]
    gain_one = norm_gains[:, 0]
    gain_two = norm_gains[:, 1]

    chosen = (my_routes[:, :, None] == jnp.arange(experts, dtype=jnp.int32)[None, None, :]).astype(full)
    flat_routes = my_routes.reshape(-1)
    route_hot = (flat_routes[:, None] == jnp.arange(experts, dtype=jnp.int32)[None, :]).astype(jnp.int32)
    before = jnp.cumsum(route_hot, axis=0) - route_hot
    slot_index = jnp.sum(before * route_hot, axis=-1)
    target = (flat_routes * capacity + slot_index).reshape(rows, 2)
    slots = experts * capacity
    slot_ids = jnp.arange(slots, dtype=jnp.int32)
    place_first = slot_ids[:, None] == target[None, :, 0]
    place_second = slot_ids[:, None] == target[None, :, 1]
    place_any = jnp.logical_or(place_first, place_second).astype(low)

    shard_in = expert_in[0].astype(low).reshape(slab, 2, grps, QUAD, units)
    in_pieces = jnp.transpose(shard_in, (1, 3, 0, 2, 4)).reshape(2, 1, QUAD, slab, quarter)
    in_pieces = jnp.broadcast_to(in_pieces, (2, grps, QUAD, slab, quarter)).reshape(
        2, reps, slab, quarter
    )
    down_mine = spread(expert_out[0].astype(low), "grp").reshape(quarter, width)
    gate_mine = swap(in_pieces[0], REP).reshape(width, quarter)
    up_mine = swap(in_pieces[1], REP).reshape(width, quarter)

    upstream = my_cotangent.astype(full) * valid_rows[:, None]

    def to_experts(block):
        sent = block.reshape((1, experts) + block.shape[1:])
        sent = jnp.broadcast_to(sent, (QUAD,) + sent.shape[1:])
        return swap(sent.reshape((QUAD * experts,) + block.shape[1:]), PLANE)

    def dispatch(values):
        return dot(place_any, values).astype(low).reshape(experts, capacity, width)

    expert_upstream = to_experts(dispatch(upstream.astype(low))).reshape(-1, width)
    active_grad_bare = lax.dot_general(
        expert_upstream, down_mine, (((1,), (1,)), ((), ())), preferred_element_type=full
    )

    x_group = group_tokens.astype(full)
    scale_group = lax.rsqrt(jnp.mean(x_group * x_group, axis=-1, keepdims=True) + eps_norm)
    normed_group = (x_group * scale_group * gain_one).astype(low).reshape(exps * rows, width)
    qkv = dot(normed_group, qkv_mine).astype(low).reshape(exps, rows, 3, heads, head_dim)
    queries = qkv[:, :, 0]
    key_rows = qkv[:, :, 1]
    values = qkv[:, :, 2]
    onehot = bucket_onehot(rows)
    bias_mine = lax.dynamic_slice_in_dim(rel_bias, place * heads, heads, 1)
    bias_table = jnp.einsum("ijb,bh->hij", onehot, bias_mine, precision=highest)

    def scores_of():
        raw = (
            jnp.einsum("sihd,sjhd->shij", queries, key_rows, preferred_element_type=full)
            * score_scale
            + bias_table[None]
        )
        return jnp.where(key_ok[:, None, None, :], raw, -1e30)

    scores = scores_of()
    row_max = jnp.max(scores, axis=-1, keepdims=True)
    log_total = row_max + jnp.log(jnp.sum(jnp.exp(scores - row_max), axis=-1, keepdims=True))
    weights_low = jnp.exp(scores - log_total).astype(low)
    context_mine = (
        jnp.einsum("shij,sjhd->sihd", weights_low, values, preferred_element_type=full)
        .astype(low)
        .reshape(exps, rows, head_cols)
    )
    context = jnp.transpose(swap(context_mine, "exp"), (1, 0, 2)).reshape(rows, width)

    x_float = tokens.astype(full)
    scale_one = lax.rsqrt(jnp.mean(x_float * x_float, axis=-1, keepdims=True) + eps_norm)
    hidden_one = x_float + dot(context, full_out)
    scale_two = lax.rsqrt(jnp.mean(hidden_one * hidden_one, axis=-1, keepdims=True) + eps_norm)
    normed_two = (hidden_one * scale_two * gain_two).astype(low)
    normed_float = normed_two.astype(full)
    router_probs = jax.nn.softmax(jnp.dot(normed_float, router, precision=highest), axis=-1)
    picked = jnp.sum(router_probs[:, None, :] * chosen, axis=-1)
    gate_total = jnp.sum(picked, axis=-1, keepdims=True)
    gate_value = picked / gate_total
    combine = gate_value * valid_rows[:, None]
    combine_slots = jnp.sum(
        jnp.where(place_first, combine[None, :, 0], 0.0)
        + jnp.where(place_second, combine[None, :, 1], 0.0),
        axis=1,
    ).reshape(experts, 1, capacity)

    expert_rows = to_experts(dispatch(normed_two)).reshape(-1, width)
    expert_combine = to_experts(combine_slots).reshape(-1, 1)

    gate_part = dot(expert_rows, gate_mine)
    up_part = dot(expert_rows, up_mine)
    active_float, active_pull = jax.vjp(gated_unit, gate_part, up_part)
    active = active_float.astype(low)
    active_scaled = (active_float * expert_combine).astype(low)
    combine_grad_part = jnp.sum(active_float * active_grad_bare, axis=-1).reshape(
        QUAD * experts, 1, capacity
    )
    gate_part_grad, up_part_grad = active_pull(active_grad_bare * expert_combine)
    gate_part_grad = gate_part_grad.astype(low)
    up_part_grad = up_part_grad.astype(low)
    rows_grad_part = (
        lax.dot_general(gate_part_grad, gate_mine, (((1,), (1,)), ((), ())), preferred_element_type=full)
        + lax.dot_general(up_part_grad, up_mine, (((1,), (1,)), ((), ())), preferred_element_type=full)
    ).astype(low)
    output_part = dot(active, down_mine).astype(low)

    combine_grad_back = swap(combine_grad_part, PLANE)
    rows_grad_back = swap(rows_grad_part.reshape(QUAD * experts, capacity, width), PLANE)
    output_back = swap(output_part.reshape(QUAD * experts, capacity, width), PLANE)

    def transposed_dot(a, b):
        return lax.dot_general(a, b, (((0,), (0,)), ((), ())), preferred_element_type=full)

    down_grad = transposed_dot(active_scaled, expert_upstream).astype(low)
    gate_grad = transposed_dot(expert_rows, gate_part_grad).astype(low)
    up_grad = transposed_dot(expert_rows, up_part_grad).astype(low)
    down_share = jnp.sum(
        swap(down_grad.reshape(grps, units, width), "grp").astype(full), axis=0
    )[None]

    def in_columns(grad):
        back = swap(grad.reshape(reps, slab, quarter), REP).astype(full)
        back = jnp.sum(back.reshape(grps, QUAD, slab, grps, units), axis=0)
        return jnp.transpose(back, (1, 2, 0, 3)).reshape(slab, grps * QUAD * units)

    in_share = jnp.concatenate([in_columns(gate_grad), in_columns(up_grad)], axis=1)[None]

    def from_slots(placed, parts):
        hot = jnp.broadcast_to(placed.astype(low)[None], (QUAD,) + placed.shape).reshape(-1, rows)
        return lax.dot_general(
            hot, parts.reshape(-1, width), (((0,), (0,)), ((), ())), preferred_element_type=full
        )

    mixture = combine[:, :1] * from_slots(place_first, output_back) + combine[:, 1:] * from_slots(
        place_second, output_back
    )
    block_loader = (valid_rows[:, None] * (hidden_one + mixture)).astype(low)
    seq_ids = jnp.arange(deal.shape[0], dtype=jnp.int32)
    dealt_seq = jnp.sum(jnp.where(deal == me, seq_ids, 0))
    block_out = lax.dynamic_index_in_dim(
        spread(block_loader, "exp"), dealt_seq - base, 0, keepdims=False
    )

    combine_grad_slots = jnp.sum(combine_grad_back.reshape(QUAD, slots), axis=0)
    combine_grad = jnp.stack(
        [
            jnp.sum(jnp.where(place_first, combine_grad_slots[:, None], 0.0), axis=0),
            jnp.sum(jnp.where(place_second, combine_grad_slots[:, None], 0.0), axis=0),
        ],
        axis=1,
    )
    gate_grad_value = combine_grad * valid_rows[:, None]
    picked_grad = (
        gate_grad_value - jnp.sum(gate_grad_value * gate_value, axis=-1, keepdims=True)
    ) / gate_total
    probs_grad = jnp.sum(picked_grad[:, :, None] * chosen, axis=1)
    logit_grad = router_probs * (
        probs_grad - jnp.sum(probs_grad * router_probs, axis=-1, keepdims=True)
    )
    router_grad = jnp.dot(normed_float.T, logit_grad, precision=highest)
    normed_grad = jnp.dot(logit_grad, router.T, precision=highest) + from_slots(
        jnp.logical_or(place_first, place_second), rows_grad_back
    )
    scaled_two = normed_grad * gain_two
    hidden_grad = (
        upstream
        + scale_two * scaled_two
        - hidden_one * scale_two**3 * jnp.mean(scaled_two * hidden_one, axis=-1, keepdims=True)
    )
    gain_two_grad = jnp.sum(normed_grad * hidden_one * scale_two, axis=0)
    branch_grad = hidden_grad.astype(low)
    context_grad = lax.dot_general(
        branch_grad, full_out, (((1,), (1,)), ((), ())), preferred_element_type=full
    ).astype(low)
    context_grad_pieces = jnp.transpose(context_grad.reshape(rows, exps, head_cols), (1, 0, 2))
    context_grad_mine = swap(context_grad_pieces, "exp").reshape(exps, rows, heads, head_dim)
    branch_group = spread(branch_grad, "exp").reshape(exps * rows, width)
    out_grad = transposed_dot(context_mine.reshape(exps * rows, head_cols), branch_group).astype(low)

    scores = scores_of()
    probs_again = jnp.exp(scores - log_total)
    weights_again = probs_again.astype(low)
    values_grad = jnp.einsum(
        "shij,sihd->sjhd", weights_again, context_grad_mine, preferred_element_type=full
    )
    probs_grad_att = jnp.einsum(
        "sihd,sjhd->shij", context_grad_mine, values, preferred_element_type=full
    )
    row_delta = jnp.sum(probs_grad_att * probs_again, axis=-1, keepdims=True)
    scores_grad = (probs_again * (probs_grad_att - row_delta)).astype(low)
    scores_grad_sum = jnp.sum(scores_grad.astype(full), axis=0)
    bias_grad_mine = jnp.einsum("hij,ijb->bh", scores_grad_sum, onehot, precision=highest)
    bias_grad = lax.dynamic_update_slice_in_dim(
        jnp.zeros((BUCKETS, HEADS), full), bias_grad_mine, place * heads, 1
    )
    queries_grad = (
        jnp.einsum("shij,sjhd->sihd", scores_grad, key_rows, preferred_element_type=full)
        * score_scale
    )
    keys_grad = (
        jnp.einsum("shij,sihd->sjhd", scores_grad, queries, preferred_element_type=full)
        * score_scale
    )
    qkv_grad = (
        jnp.stack([queries_grad, keys_grad, values_grad], axis=2)
        .astype(low)
        .reshape(exps * rows, 3 * head_cols)
    )
    normed_one_part = lax.dot_general(
        qkv_grad, qkv_mine, (((1,), (1,)), ((), ())), preferred_element_type=full
    ).astype(low)
    normed_one_grad = jnp.sum(
        swap(normed_one_part.reshape(exps, rows, width), "exp").astype(full), axis=0
    )
    scaled_one = normed_one_grad * gain_one
    token_grad = (
        hidden_grad
        + scale_one * scaled_one
        - x_float * scale_one**3 * jnp.mean(scaled_one * x_float, axis=-1, keepdims=True)
    )
    gain_one_grad = jnp.sum(normed_one_grad * x_float * scale_one, axis=0)

    qkv_weight_grad = transposed_dot(normed_group, qkv_grad).astype(low)
    qkv_grad_rows = swap(qkv_weight_grad.reshape(exps, row_block, 3 * head_cols), "exp")
    qkv_grad_rows = jnp.transpose(
        qkv_grad_rows.reshape(exps, row_block, 3, head_cols), (1, 2, 0, 3)
    ).reshape(row_block, reps, -1)
    qkv_share = jnp.sum(
        swap(jnp.transpose(qkv_grad_rows, (1, 0, 2)), REP).astype(full), axis=0
    )
    out_pieces = jnp.transpose(out_grad.reshape(row_block, reps, -1), (1, 0, 2))
    out_share = jnp.sum(swap(out_pieces, REP).astype(full), axis=0)

    small = jnp.concatenate(
        [
            router_grad.reshape(-1),
            jnp.stack([gain_one_grad, gain_two_grad], axis=1).reshape(-1),
            bias_grad.reshape(-1),
        ]
    ).reshape(-1, 128)
    small_total = jnp.sum(lax.all_gather(small, ALL, axis=0, tiled=False), axis=0).reshape(-1)
    router_total = small_total[: router.size].reshape(router.shape)
    gains_total = small_total[router.size : router.size + norm_gains.size].reshape(norm_gains.shape)
    bias_total = small_total[router.size + norm_gains.size :].reshape(rel_bias.shape)

    qkv_new = adamw_update(attn_qkv, qkv_first, qkv_second, qkv_share, 1.5 / math.sqrt(D), 0.1)
    out_new = adamw_update(attn_out, out_first, out_second, out_share, 6.0 / math.sqrt(D), 0.1)
    bias_new = adamw_update(rel_bias, bias_first, bias_second, bias_total, 0.3, 0.0)
    router_new = adamw_update(
        router, router_first, router_second, router_total, 1.0 / math.sqrt(D), 0.1
    )
    gains_new = adamw_update(norm_gains, gains_first, gains_second, gains_total, 0.5, 0.0)
    in_new = adamw_update(expert_in, in_first, in_second, in_share, 1.5 / math.sqrt(D), 0.1)
    down_new = adamw_update(
        expert_out, down_first, down_second, down_share, 1.5 / math.sqrt(FF), 0.1
    )
    return (
        (block_out, token_grad)
        + qkv_new
        + out_new
        + bias_new
        + router_new
        + gains_new
        + in_new
        + down_new
    )


def solution(mesh):
    reps, exps = mesh.devices.shape
    split = Mesh(mesh.devices.reshape(reps // QUAD, QUAD, exps), ALL)
    by_rows = P(ALL, None)
    attn = P("exp", REP)
    expert = P("exp", REP, None)
    return jax.shard_map(
        per_device if (reps, exps) == (2 * QUAD, 4) else plain_device,
        mesh=split,
        in_specs=(by_rows, by_rows) + (P(),) * 3 + (attn,) * 6 + (P(),) * 9 + (expert,) * 6,
        out_specs=(by_rows, by_rows) + (attn,) * 6 + (P(),) * 9 + (expert,) * 6,
        check_vma=False,
    )
```

```python
import functools
import math

import jax
import jax.numpy as jnp
from jax import lax
from jax.experimental import pallas as pl
from jax.experimental.pallas import tpu as pltpu
from jax.sharding import Mesh
from jax.sharding import PartitionSpec as P

D = 1024
HEADS = 16
FF = 2816
BUCKETS = 32
STEP = 10
QUAD = 4
REP = ("grp", "quad")
PLANE = ("quad", "exp")
ALL = ("grp", "quad", "exp")

highest = lax.Precision.HIGHEST
eps_norm = 1e-06
thresholds = (1, 2, 3, 4, 5, 6, 7, 8, 11, 16, 22, 32, 45, 64, 90)
beta_one = 0.9
beta_two = 0.999
eps_adam = 1e-08
low = jnp.bfloat16
full = jnp.float32
MESH = pl.DeviceIdType.MESH


def adamw_update(weight, moment, second, gradient, step_rate, decay_factor):
    new_moment = beta_one * moment + (1.0 - beta_one) * gradient
    new_second = beta_two * second + (1.0 - beta_two) * gradient * gradient
    corrected = new_moment / (1.0 - beta_one**STEP)
    scaled = new_second / (1.0 - beta_two**STEP)
    new_weight = weight - step_rate * (
        corrected / (jnp.sqrt(scaled) + eps_adam) + decay_factor * weight
    )
    return (new_moment, new_second, new_weight)


def gated_unit(gate_input, up_input):
    return jax.nn.gelu(gate_input, approximate=True) * up_input


def dot(a, b):
    return jnp.dot(a, b, preferred_element_type=full)


def nt(a, b, precision=None):
    return lax.dot_general(a, b, (((1,), (1,)), ((), ())), preferred_element_type=full, precision=precision)


def tn(a, b):
    return lax.dot_general(a, b, (((0,), (0,)), ((), ())), preferred_element_type=full)


class Where:
    def __init__(self, grps, exps):
        self.grps, self.exps = grps, exps
        self.reps = grps * QUAD
        self.grp = lax.axis_index("grp")
        self.quad = lax.axis_index("quad")
        self.exp = lax.axis_index("exp")
        self.rep = self.grp * QUAD + self.quad
        self.base = self.rep * exps
        self.me = self.base + self.exp

    def device(self, rep, exp):
        return (rep // QUAD, rep % QUAD, exp)

    def near(self, flip):
        q = self.quad
        if flip & 1:
            q = q + 1 - 2 * (q % 2)
        if flip & 2:
            q = q + 2 - 4 * (q // 2)
        return q


def send(src, dst, send_sem, recv_sem, device):
    return pltpu.make_async_remote_copy(
        src_ref=src, dst_ref=dst, send_sem=send_sem, recv_sem=recv_sem, device_id=device, device_id_type=MESH
    )


def arrived(ref, sem):
    pltpu.make_async_copy(ref, ref, sem).wait()


def greet(count, device):
    barrier = pltpu.get_barrier_semaphore()

    def one(k, _):
        pl.semaphore_signal(barrier, inc=1, device_id=device(k), device_id_type=MESH)
        return 0

    lax.fori_loop(1, count + 1, one, 0)
    return functools.partial(pl.semaphore_wait, barrier, count)


def everyone(at):
    count = at.reps * at.exps

    def device(k):
        other = (at.me + k) % count
        return at.device(other // at.exps, other % at.exps)

    return count - 1, device


def neighbours(at):
    members = QUAD * at.exps
    plane = at.quad * at.exps + at.exp

    def device(k):
        other = (plane + k) % members
        rest = k - members
        grp = jnp.where(k < members, at.grp, (at.grp + 1 + rest // QUAD) % at.grps)
        quad = jnp.where(k < members, other // at.exps, rest % QUAD)
        return grp, quad, jnp.where(k < members, other % at.exps, at.exp)

    return members - 1 + QUAD * (at.grps - 1), device


def turn(exp, i):
    beside = exp + 1 - 2 * (exp % 2)
    return jnp.where(i == 0, (beside + 2) % 4, jnp.where(i == 1, (exp + 2) % 4, jnp.where(i == 2, beside, exp)))


def lane_of(shape):
    return lax.broadcasted_iota(jnp.int32, shape, 1)


def row_of(shape):
    return lax.broadcasted_iota(jnp.int32, shape, 0)


def bucket_of(offset):
    distance = jnp.abs(offset)
    bucket = jnp.where(offset > 0, 16, 0)
    for threshold in thresholds:
        bucket = bucket + jnp.where(distance >= threshold, 1, 0)
    return bucket


def bits_of(count):
    return count.bit_length() - 1


def column_parts(width):
    tiles = width // 128
    cuts = [0, (tiles + 2) // 3, (2 * tiles + 2) // 3, tiles]
    return [(cuts[i] * 128, (cuts[i + 1] - cuts[i]) * 128) for i in range(3)]


def flipped(place, bit):
    return place + (1 - 2 * ((place // (1 << bit)) % 2)) * (1 << bit)


class Doubling:
    def __init__(self, at, own, every, sems, core_sems, orders):
        self.at, self.own, self.every = at, own, every
        self.sems, self.core_sems, self.orders = sems, core_sems, orders
        self.plane = at.quad * at.exps + at.exp
        self.steps = len(orders[0])
        self.parts = column_parts(own.shape[1])

    def device(self, bit):
        other = flipped(self.plane, bit)
        return (self.at.grp, other // self.at.exps, other % self.at.exps)

    def place(self, part, j):
        p = self.plane
        for i, bit in enumerate(self.orders[part]):
            if (j >> i) & 1:
                p = flipped(p, bit + 1)
        return p

    def block(self, part, p):
        begin, size = self.parts[part]
        return self.every.at[p, :, pl.ds(begin, size)]

    def source(self, part, j):
        begin, size = self.parts[part]
        return self.own.at[:, pl.ds(begin, size)] if j == 0 else self.block(part, self.place(part, j))

    def index(self, step, part, j):
        return part * (1 << self.steps) + (1 << step) - 1 + j

    def copy(self, step, part, j):
        i = self.index(step, part, j)
        return send(
            self.source(part, j),
            self.block(part, self.place(part, j)),
            self.sems.at[0, i],
            self.sems.at[1, i],
            self.device(self.orders[part][step] + 1),
        )

    def core_copy(self, part, j):
        i = part * (1 << self.steps) + j
        return send(
            self.source(part, j),
            self.block(part, self.place(part, j)),
            self.core_sems.at[0, i],
            self.core_sems.at[1, i],
            self.device(0),
        )

    def start(self):
        for part in range(3):
            for step in range(self.steps):
                self.copy(step, part, 0).start()
        for part in range(3):
            self.core_copy(part, 0).start()
        self.keep().start()

    def keep(self):
        return pltpu.make_async_copy(self.own, self.every.at[self.plane], self.core_sems.at[1, 3 << self.steps])

    def next(self, step):
        for part in range(3):
            for j in range(1 << step):
                k = (1 << step) + j
                arrived(self.block(part, self.place(part, k)), self.sems.at[1, self.index(step, part, j)])
                for later in range(step + 1, self.steps):
                    self.copy(later, part, k).start()
                self.core_copy(part, k).start()

    def finish_in(self):
        for part in range(3):
            for j in range(1 << self.steps):
                there = self.block(part, flipped(self.place(part, j), 0))
                arrived(there, self.core_sems.at[1, part * (1 << self.steps) + j])
        self.keep().wait()

    def finish_out(self):
        for part in range(3):
            for j in range(1 << self.steps):
                self.core_copy(part, j).wait_send()
            for step in range(self.steps):
                for j in range(1 << step):
                    self.copy(step, part, j).wait_send()


class Halving:
    def __init__(self, at, bufs, sems, orders):
        self.at, self.bufs, self.sems = at, bufs, sems
        self.plane = at.quad * at.exps + at.exp
        self.places = bits_of(QUAD * at.exps)
        self.chip_bits = list(range(self.places - 1))
        self.parts = column_parts(bufs[0].shape[2])
        self.orders = orders

    def device(self, bit):
        other = flipped(self.plane, bit)
        return (self.at.grp, other // self.at.exps, other % self.at.exps)

    def hop(self, step, part):
        order = self.orders[part]
        bit = order[step]
        left = [b for b in self.chip_bits if b not in order[:step]]
        pos = left.index(bit)
        half = 1 << (len(left) - 1)
        mine = (self.plane // (1 << (bit + 1))) % 2
        device = self.device(bit + 1)
        begin, size = self.parts[part]
        cols = pl.ds(begin, size)
        base = self.base(step, part)

        def index(j, value):
            return (j >> pos) * (1 << (pos + 1)) + value * (1 << pos) + j % (1 << pos)

        pairs = []
        for j in range(half):
            copy = functools.partial(
                send,
                self.bufs[step].at[index(j, 1 - mine), :, cols],
                self.bufs[step + 1].at[j, :, cols],
                self.sems.at[0, base + j],
                self.sems.at[1, base + j],
                device,
            )
            pairs.append((copy, index(j, mine), j))
        return pairs, begin, size, base

    def base(self, step, part):
        n = len(self.chip_bits)
        return part * (1 << n) + sum(1 << (n - 1 - s) for s in range(step))

    def start(self, step, part=None):
        for p in range(3) if part is None else [part]:
            for copy, _, _ in self.hop(step, p)[0]:
                copy().start()

    def add(self, step, part):
        pairs, begin, size, base = self.hop(step, part)
        cols = pl.ds(begin, size)
        here, there = self.bufs[step], self.bufs[step + 1]
        for _, keep, j in pairs:
            arrived(there.at[j, :, cols], self.sems.at[1, base + j])
            there[j, :, begin : begin + size] = (
                there[j, :, begin : begin + size] + here[keep, :, begin : begin + size]
            )

    def next(self, step):
        for p in range(3):
            self.add(step, p)
            if step + 1 < len(self.chip_bits):
                self.start(step + 1, p)

    def result(self):
        return self.bufs[len(self.chip_bits)]

    def finish(self):
        for step in range(len(self.chip_bits)):
            for p in range(3):
                for copy, _, _ in self.hop(step, p)[0]:
                    copy().wait_send()


class Group:
    def __init__(self, at, own, every, sems):
        self.at, self.own, self.every, self.sems = at, own, every, sems
        self.beside, self.across = at.exp + 1 - 2 * (at.exp % 2), (at.exp + 2) % 4

    def copy(self, src, index, send_index, device):
        return send(
            src, self.every.at[index], self.sems.at[0, send_index], self.sems.at[1, index], self.at.device(self.at.rep, device)
        )

    def first(self):
        return [
            self.copy(self.own, self.at.exp, 0, self.across),
            self.copy(self.own, self.at.exp, 1, self.beside),
        ]

    def second(self):
        return self.copy(self.every.at[self.across], self.across, 2, self.beside)

    def start(self):
        for copy in self.first():
            copy.start()

    def pass_on(self):
        arrived(self.every.at[self.across], self.sems.at[1, self.across])
        self.second().start()

    def arrive(self):
        for index in (self.beside, (self.beside + 2) % 4):
            arrived(self.every.at[index], self.sems.at[1, index])

    def sent(self):
        for copy in self.first() + [self.second()]:
            copy.wait_send()


class Tiles:
    def __init__(self, units, reps):
        self.units = units
        self.reps = reps
        self.hidden = units * reps
        self.half = self.hidden // 256
        self.wide = (self.half + 1) // 2
        self.count = 3
        self.size = 128 * self.wide // self.count
        self.skip = 128 * (2 * self.wide - self.half)

    def start(self, quad):
        return 128 * (self.half * (quad // 2) + (self.half - self.wide) * (quad % 2))

    def rows(self, tile):
        result = []
        for k in range(QUAD):
            found = None
            for parity in range(2):
                first = self.start(parity) + tile * self.size
                live = first + (self.skip if parity and tile == 0 else 0)
                begin = max(live, k * self.units)
                end = min(first + self.size, (k + 1) * self.units)
                if end > begin:
                    found = (begin - k * self.units, end - begin, parity, begin - first)
            result.append(found)
        return result


class Outward:
    def __init__(self, at, tiles, tile, in_low, down_slab, both_w, down_w, nothing, sems, down_sems):
        self.at, self.tiles, self.tile = at, tiles, tile
        self.in_low, self.down_slab, self.both_w, self.down_w = in_low, down_slab, both_w, down_w
        self.nothing, self.sems, self.down_sems = nothing, sems, down_sems
        self.slab = in_low.shape[0]

    def source(self, quad, section):
        begin = section * self.tiles.hidden + self.tiles.start(quad) + self.tile * self.tiles.size
        return self.in_low.at[:, pl.ds(pl.multiple_of(begin, 128), self.tiles.size)]

    def target(self, rep, section):
        rows = pl.ds(pl.multiple_of(rep * self.slab, self.slab), self.slab)
        return self.both_w.at[rows, pl.ds(section * self.tiles.size, self.tiles.size)]

    def over(self, act):
        at = self.at

        def one(k, _):
            other = (at.rep + k) % at.reps
            for section in range(2):
                act(
                    functools.partial(
                        send,
                        self.source(other % QUAD, section),
                        self.target(at.rep, section),
                        self.sems.at[0, section * at.reps + other],
                        self.sems.at[1, section * at.reps + at.rep],
                        at.device(other, at.exp),
                    )
                )
            return 0

        lax.fori_loop(1, at.reps, one, 0)

    def over_down(self, act, act_local):
        at = self.at
        for k, piece in enumerate(self.tiles.rows(self.tile)):
            if piece is None:
                continue
            begin, count, parity, to = piece
            quad = 2 * (at.rep // QUAD) + parity
            src, dst = self.down_slab.at[pl.ds(begin, count)], self.down_w.at[pl.ds(to, count)]
            recv = self.down_sems.at[1, at.rep]
            for g in range(at.grps):
                stays = jnp.logical_and(at.grp == g, at.quad == quad)
                ours = at.rep % QUAD == k

                @pl.when(jnp.logical_and(ours, jnp.logical_not(stays)))
                def _():
                    act(functools.partial(send, src, dst, self.down_sems.at[0, g], recv, (g, quad, at.exp)))

                @pl.when(jnp.logical_and(ours, stays))
                def _():
                    act_local(functools.partial(pltpu.make_async_copy, src, dst, recv))

    def blank(self):
        return pltpu.make_async_copy(
            self.nothing, self.down_w.at[pl.ds(0, self.tiles.skip)], self.down_sems.at[1, self.at.reps]
        )

    def start(self):
        at = self.at
        self.over_down(lambda copy: copy().start(), lambda copy: copy().start())
        self.over(lambda copy: copy().start())
        for section in range(2):
            pltpu.make_async_copy(
                self.source(at.quad, section), self.target(at.rep, section), self.sems.at[1, section * at.reps + at.rep]
            ).start()
        if self.tile == 0:

            @pl.when(at.quad % 2 == 1)
            def _():
                self.blank().start()

    def arrive(self):
        at = self.at

        def one(rep, _):
            for section in range(2):
                arrived(self.target(rep, section), self.sems.at[1, section * at.reps + rep])
            return 0

        lax.fori_loop(0, at.reps, one, 0)
        for parity in range(2):

            @pl.when(at.quad % 2 == parity)
            def _():
                for k, piece in enumerate(self.tiles.rows(self.tile)):
                    if piece is not None and piece[2] == parity:
                        source = QUAD * (at.quad // 2) + k
                        arrived(self.down_w.at[pl.ds(piece[3], piece[1])], self.down_sems.at[1, source])
                if parity and self.tile == 0:
                    self.blank().wait()

    def sent(self):
        self.over(lambda copy: copy().wait_send())
        self.over_down(lambda copy: copy().wait_send(), lambda copy: None)


class Homeward:
    def __init__(self, at, tiles, tile, both, down, in_parts, down_parts, sems, down_sems, sections=(0, 1)):
        self.at, self.tiles, self.tile, self.sections = at, tiles, tile, sections
        self.both, self.down, self.in_parts, self.down_parts = both, down, in_parts, down_parts
        self.sems, self.down_sems = sems, down_sems
        self.slab = in_parts.shape[1]

    def target(self, grp, quad, parity, section):
        skip = self.tiles.skip if parity and self.tile == 0 else 0
        to = section * self.tiles.hidden + self.tiles.start(quad) + self.tile * self.tiles.size + skip
        to = to if isinstance(to, int) else pl.multiple_of(to, 128)
        return skip, self.in_parts.at[grp, :, pl.ds(to, self.tiles.size - skip)]

    def copy(self, rep, parity, section, local=False):
        at = self.at
        skip, dst = self.target(at.grp, at.quad, parity, section)
        rows = pl.ds(pl.multiple_of(rep * self.slab, self.slab), self.slab)
        src = self.both.at[rows, pl.ds(section * self.tiles.size + skip, self.tiles.size - skip)]
        recv = self.sems.at[1, section * at.reps + at.rep]
        if local:
            return pltpu.make_async_copy(src, dst, recv)
        return send(src, dst, self.sems.at[0, section * at.reps + rep], recv, at.device(rep, at.exp))

    def over(self, act, act_local):
        at = self.at
        for parity in range(2):

            @pl.when(at.quad % 2 == parity)
            def _():
                def one(k, _):
                    for section in self.sections:
                        act(self.copy((at.rep + k) % at.reps, parity, section))
                    return 0

                lax.fori_loop(1, at.reps, one, 0)
                if act_local:
                    for section in self.sections:
                        act_local(self.copy(at.rep, parity, section, local=True))

    def over_down(self, act, act_local):
        at = self.at
        if self.down is None:
            return
        for k, piece in enumerate(self.tiles.rows(self.tile)):
            if piece is None:
                continue
            begin, count, parity, to = piece
            src, dst = self.down.at[pl.ds(to, count)], self.down_parts.at[at.grp, pl.ds(begin, count)]
            recv = self.down_sems.at[1, at.grp]
            stays = jnp.logical_and(at.grp == at.quad // 2, at.quad == k)
            ours = at.quad % 2 == parity

            @pl.when(jnp.logical_and(ours, jnp.logical_not(stays)))
            def _():
                act(functools.partial(send, src, dst, self.down_sems.at[0, k], recv, (at.quad // 2, k, at.exp)))

            @pl.when(jnp.logical_and(ours, stays))
            def _():
                act_local(functools.partial(pltpu.make_async_copy, src, dst, recv))

    def start(self):
        self.over_down(lambda copy: copy().start(), lambda copy: copy().start())
        self.over(lambda copy: copy.start(), lambda copy: copy.start())

    def arrive(self):
        at = self.at
        for rep in range(at.reps):
            for section in self.sections:
                _, dst = self.target(rep // QUAD, rep % QUAD, rep % 2, section)
                arrived(dst, self.sems.at[1, section * at.reps + rep])
        for k, piece in enumerate(self.tiles.rows(self.tile)):
            if piece is None or self.down is None:
                continue

            @pl.when(at.quad == k)
            def _():
                for g in range(at.grps):
                    arrived(self.down_parts.at[g, pl.ds(piece[0], piece[1])], self.down_sems.at[1, g])

    def sent(self):
        self.over(lambda copy: copy.wait_send(), None)
        self.over_down(lambda copy: copy().wait_send(), lambda copy: None)


def forward_kernel(
    grps,
    exps,
    lengths,
    bias_table,
    routes_t,
    tokens,
    cotangent,
    gains,
    router,
    attn_qkv,
    attn_out,
    expert_in,
    expert_out,
    both_w,
    down_w,
    cot_all,
    n_all,
    comb_all,
    qkv_out,
    pb_out,
    mine_out,
    n1_out,
    wqkv_out,
    wout_out,
    h1_out,
    n2_out,
    probs_out,
    in_out,
    down_out,
    in_wide,
    down_wide,
    qkv_t,
    out_w,
    in_low,
    down_slab,
    tok_all,
    wqkv,
    wout,
    n1,
    qkv,
    pb,
    mine,
    ctx,
    bias,
    comb_send,
    nothing,
    tok_sem,
    wq_sem,
    wo_sem,
    wo2_sem,
    weight_sem,
    down_sem,
    ctx_sem,
    cot_sem,
    cot_core_sem,
    n_sem,
    n_core_sem,
    comb_sem,
    store_sem,
    cast_sem,
):
    at = Where(grps, exps)
    reps = at.reps
    rows, width = tokens.shape
    heads = HEADS // exps
    head_dim = width // HEADS
    head_cols = heads * head_dim
    block_cols = min(128, head_cols)
    shard_cols, row_block = qkv_t.shape
    seg = math.gcd(shard_cols, head_cols)
    segs = shard_cols // seg
    tiles = Tiles(down_slab.shape[0], reps)
    plane = at.quad * exps + at.exp
    members = QUAD * exps
    scale = 1.0 / math.sqrt(head_dim)
    SEND, RECV = 0, 1

    met = greet(*everyone(at))
    wide_copies = [
        pltpu.make_async_copy(expert_in, in_wide, cast_sem.at[0]),
        pltpu.make_async_copy(expert_out, down_wide, cast_sem.at[1]),
    ]
    for copy in wide_copies:
        copy.start()
    qkv_t[...] = attn_qkv[...].T.astype(low)
    out_w[...] = attn_out[...].astype(low)
    met()

    def exp_peer(k):
        return (at.exp + k) % exps

    group_tokens = Group(at, tokens, tok_all, tok_sem)
    group_tokens.start()
    tok_all[at.exp] = tokens[...]

    def segment(k):
        col = (at.rep * segs + k) * seg
        section = col // width
        within = col - section * width
        owner = within // head_cols
        return owner, section * head_cols + within - owner * head_cols

    def segment_copy(k, shift):
        owner, offset = segment(k)
        src = qkv_t.at[pl.ds(k * seg, seg)]
        dst = wqkv.at[at.exp, pl.ds(pl.multiple_of(offset, seg), seg)]
        target = at.device((at.rep + shift) % reps, owner)
        return owner, src, dst, functools.partial(
            send, src, dst, wq_sem.at[SEND, k * reps + shift], wq_sem.at[RECV, at.exp * 3 * (head_cols // seg) + offset // seg], target
        )

    def over_segments(act, act_local):
        def one(i, _):
            k, shift = i // reps, i % reps
            owner, src, dst, copy = segment_copy(k, shift)
            stays = jnp.logical_and(shift == 0, owner == at.exp)

            @pl.when(jnp.logical_not(stays))
            def _():
                act(copy())

            @pl.when(stays)
            def _():
                act_local(k, src, dst)

            return 0

        lax.fori_loop(0, segs * reps, one, 0)

    def local_segment(k, src, dst):
        _, offset = segment(k)
        pltpu.make_async_copy(src, dst, wq_sem.at[RECV, at.exp * 3 * (head_cols // seg) + offset // seg]).start()

    over_segments(lambda copy: copy.start(), local_segment)

    span = 2 * rows
    bucket = bucket_of(lane_of((8, span)) - rows)
    for h in range(heads):
        line = jnp.zeros((8, span), full)
        for b in range(BUCKETS):
            line = jnp.where(bucket == b, bias_table[at.exp * heads + h, b], line)
        whole = jnp.broadcast_to(line[0:1], (rows, span))
        bias[h] = pltpu.roll(whole, 0, 1, stride=1, stride_axis=0)[:, rows:]

    group_tokens.pass_on()
    group_tokens.arrive()

    def norm_group(s, _):
        x = tok_all[s].astype(full)
        r = lax.rsqrt(jnp.mean(x * x, axis=1, keepdims=True) + eps_norm)
        n1[s] = (x * r * gains[0:1, :]).astype(low)
        return 0

    lax.fori_loop(0, exps, norm_group, 0)

    for k in range(1, reps):
        other = (at.rep + k) % reps
        send(
            out_w, wout.at[at.exp, at.rep], wo_sem.at[SEND, other], wo_sem.at[RECV, at.rep], at.device(other, at.exp)
        ).start()
    wout[at.exp, at.rep] = out_w[...]
    chip_bits = list(range(bits_of(members) - 1))
    cots = Doubling(at, cotangent, cot_all, cot_sem, cot_core_sem, [chip_bits[::-1]] * 3)
    cots.start()

    for copy in wide_copies:
        copy.wait()
    in_low[...] = in_wide[...].astype(low)
    down_slab[...] = down_wide[...].astype(low)
    nothing[...] = jnp.zeros_like(nothing)
    weights = [
        Outward(
            at, tiles, t, in_low, down_slab, both_w.at[t], down_w.at[t], nothing, weight_sem.at[t], down_sem.at[t]
        )
        for t in range(2)
    ]

    def wait_segment(i, _):
        e, j = i // (3 * head_cols // seg), i % (3 * head_cols // seg)
        arrived(wqkv.at[e, pl.ds(pl.multiple_of(j * seg, seg), seg)], wq_sem.at[RECV, i])
        return 0

    lax.fori_loop(0, exps * 3 * head_cols // seg, wait_segment, 0)

    weights[0].start()

    def project(s, _):
        total = jnp.zeros((rows, 3 * head_cols), full)
        for e in range(exps):
            total = total + nt(n1[s, :, e * row_block : (e + 1) * row_block], wqkv[e])
        qkv[s] = total.astype(low)
        return 0

    lax.fori_loop(0, exps, project, 0)

    group_wout = Group(at, wout.at[at.exp], wout, wo2_sem)

    def beside(k):
        if k == 1:
            for j in range(1, reps):
                other = (at.rep + j) % reps
                arrived(wout.at[at.exp, other], wo_sem.at[RECV, other])
            group_wout.start()
        elif k == 2:
            cots.next(0)
        else:
            group_wout.pass_on()

    def attend(i, _):
        s = turn(at.exp, i)
        for k in range(1, exps):

            @pl.when(i == k)
            def _():
                beside(k)

        ok = lane_of((rows, rows)) < lengths[at.base + s]
        lane = lane_of((rows, block_cols))
        for c in range(head_cols // block_cols):
            cols = slice(c * block_cols, (c + 1) * block_cols)
            q = qkv[s, :, cols] * scale
            k = qkv[s, :, head_cols + c * block_cols : head_cols + (c + 1) * block_cols]
            v = qkv[s, :, 2 * head_cols + c * block_cols : 2 * head_cols + (c + 1) * block_cols]
            result = jnp.zeros((rows, block_cols), full)
            for t in range(block_cols // head_dim):
                h = c * (block_cols // head_dim) + t
                here = jnp.logical_and(lane >= t * head_dim, lane < (t + 1) * head_dim)
                scores = nt(jnp.where(here, q, jnp.zeros_like(q)), k) + bias[h]
                scores = jnp.where(ok, scores, -1e30)
                top = jnp.max(scores, axis=1, keepdims=True)
                weights = jnp.exp(scores - top)
                total = jnp.sum(weights, axis=1, keepdims=True)
                weights = (weights * (1.0 / total)).astype(low)
                result = jnp.where(here, jnp.dot(weights, v, preferred_element_type=full), result)
                pb[s * heads + h] = weights
            mine[s, :, cols] = result.astype(low)

        @pl.when(i < exps - 1)
        def _():
            send(
                mine.at[s], ctx.at[at.exp], ctx_sem.at[SEND, s], ctx_sem.at[RECV, at.exp], at.device(at.rep, s)
            ).start()

        @pl.when(i == exps - 1)
        def _():
            pltpu.make_async_copy(mine.at[s], ctx.at[at.exp], ctx_sem.at[RECV, at.exp]).start()

        return 0

    lax.fori_loop(0, exps, attend, 0)

    cots.next(1)
    group_wout.arrive()
    for e in range(exps):
        arrived(ctx.at[e], ctx_sem.at[RECV, e])

    out_cols = wout.shape[3]
    for r in range(reps):
        cols = slice(r * out_cols, (r + 1) * out_cols)
        total = tokens[:, cols].astype(full)
        for e in range(exps):
            total = total + jnp.dot(ctx[e], wout[e, r], preferred_element_type=full)
        h1_out[:, cols] = total
    h1 = h1_out[...]
    r2 = lax.rsqrt(jnp.mean(h1 * h1, axis=1, keepdims=True) + eps_norm)
    n2 = (h1 * r2 * gains[1:2, :]).astype(low)
    n2_out[...] = n2
    rotated = [chip_bits[c:] + chip_bits[:c] for c in range(3)]
    rows_two = Doubling(at, n2_out, n_all, n_sem, n_core_sem, rotated)
    rows_two.start()
    weights[1].start()

    router_rows = jnp.concatenate([router[...], jnp.zeros((128 - exps, width), full)], axis=0)
    logits = nt(n2.astype(full), router_rows, precision=highest)
    lane = lane_of((rows, 128))
    logits = jnp.where(lane < exps, logits, -1e30)
    probs = jnp.exp(logits - jnp.max(logits, axis=1, keepdims=True))
    probs = probs / jnp.sum(probs, axis=1, keepdims=True)
    probs_out[...] = probs
    picked = jnp.where(routed(routes_t, at.me, rows), probs, 0.0)
    comb = picked / jnp.sum(picked, axis=1, keepdims=True)
    comb = jnp.where(row_of((rows, 1)) < lengths[at.me], comb, 0.0)
    comb_send[...] = comb.T[0 : comb_send.shape[0]]

    def comb_copy(k):
        other = (plane + k) % members
        return send(
            comb_send,
            comb_all.at[plane],
            comb_sem.at[SEND, other],
            comb_sem.at[RECV, plane],
            (at.grp, other // exps, other % exps),
        )

    def start_comb(k, _):
        comb_copy(k).start()
        return 0

    lax.fori_loop(1, members, start_comb, 0)
    pltpu.make_async_copy(comb_send, comb_all.at[plane], comb_sem.at[RECV, plane]).start()
    rows_two.next(0)

    stores = [
        (qkv, qkv_out),
        (pb, pb_out),
        (mine, mine_out),
        (n1, n1_out),
        (wqkv, wqkv_out),
        (wout, wout_out),
        (in_low, in_out),
        (down_slab, down_out),
    ]
    for i, (src, dst) in enumerate(stores):
        pltpu.make_async_copy(src, dst, store_sem.at[i]).start()

    for step in range(1, rows_two.steps):
        rows_two.next(step)
    for step in range(2, cots.steps):
        cots.next(step)

    cots.finish_in()
    rows_two.finish_in()

    def comb_in(k, _):
        arrived(comb_all.at[k], comb_sem.at[RECV, k])
        return 0

    lax.fori_loop(0, members, comb_in, 0)
    for tile in weights:
        tile.arrive()

    for k in range(1, exps):
        peer = exp_peer(k)
        arrived(mine.at[peer], ctx_sem.at[SEND, peer])
    over_segments(lambda copy: copy.wait_send(), lambda k, src, dst: None)
    for k in range(1, reps):
        arrived(out_w, wo_sem.at[SEND, (at.rep + k) % reps])
    group_tokens.sent()
    group_wout.sent()
    cots.finish_out()
    rows_two.finish_out()

    def sent_comb(k, _):
        comb_copy(k).wait_send()
        return 0

    lax.fori_loop(1, members, sent_comb, 0)
    for tile in weights:
        tile.sent()
    for i, (src, dst) in enumerate(stores):
        pltpu.make_async_copy(src, dst, store_sem.at[i]).wait()


def forward_call(
    grps, exps, lengths, bias_table, routes_t, tokens, cotangent, gains, router, attn_qkv, attn_out, expert_in, expert_out
):
    reps = grps * QUAD
    rows, width = tokens.shape
    head_cols = width // exps
    row_block, shard_cols = attn_qkv.shape
    seg = math.gcd(shard_cols, head_cols)
    segs = shard_cols // seg
    units = expert_out.shape[0]
    out_cols = attn_out.shape[1]
    heads = HEADS // exps
    members = QUAD * exps
    tiles = Tiles(units, reps)
    shape = jax.ShapeDtypeStruct
    vmem = pl.BlockSpec(memory_space=pltpu.VMEM)
    smem = pl.BlockSpec(memory_space=pltpu.SMEM)
    hbm = pl.BlockSpec(memory_space=pl.ANY)
    results = [
        (shape((2, width, 2 * tiles.size), low), hbm),
        (shape((2, tiles.size, width), low), hbm),
        (shape((members, rows, width), low), hbm),
        (shape((members, rows, width), low), hbm),
        (shape((members, 8, rows), full), hbm),
        (shape((exps, rows, 3 * head_cols), low), hbm),
        (shape((exps * heads, rows, rows), low), hbm),
        (shape((exps, rows, head_cols), low), hbm),
        (shape((exps, rows, width), low), hbm),
        (shape((exps, 3 * head_cols, row_block), low), hbm),
        (shape((exps, reps, row_block, out_cols), low), hbm),
        (shape((rows, width), full), vmem),
        (shape((rows, width), low), vmem),
        (shape((rows, 128), full), vmem),
        (shape(expert_in.shape, low), hbm),
        (shape(expert_out.shape, low), hbm),
    ]
    dma = pltpu.SemaphoreType.DMA
    chips = members // 2
    return pl.pallas_call(
        functools.partial(forward_kernel, grps, exps),
        out_shape=[r[0] for r in results],
        in_specs=[smem] * 2 + [vmem] * 7 + [hbm] * 2,
        out_specs=[r[1] for r in results],
        scratch_shapes=[
            pltpu.VMEM(expert_in.shape, full),
            pltpu.VMEM(expert_out.shape, full),
            pltpu.VMEM((shard_cols, row_block), low),
            pltpu.VMEM((row_block, out_cols), low),
            pltpu.VMEM(expert_in.shape, low),
            pltpu.VMEM(expert_out.shape, low),
            pltpu.VMEM((exps, rows, width), low),
            pltpu.VMEM((exps, 3 * head_cols, row_block), low),
            pltpu.VMEM((exps, reps, row_block, out_cols), low),
            pltpu.VMEM((exps, rows, width), low),
            pltpu.VMEM((exps, rows, 3 * head_cols), low),
            pltpu.VMEM((exps * heads, rows, rows), low),
            pltpu.VMEM((exps, rows, head_cols), low),
            pltpu.VMEM((exps, rows, head_cols), low),
            pltpu.VMEM((heads, rows, rows), full),
            pltpu.VMEM((8, rows), full),
            pltpu.VMEM((tiles.skip, width), low),
            dma((2, exps)),
            dma((2, max(segs * reps, exps * 3 * head_cols // seg))),
            dma((2, reps)),
            dma((2, exps)),
            dma((2, 2, 2 * reps)),
            dma((2, 2, reps + 1)),
            dma((2, exps)),
            dma((2, 3 * chips)),
            dma((2, 3 * chips + 1)),
            dma((2, 3 * chips)),
            dma((2, 3 * chips + 1)),
            dma((2, members)),
            dma((8,)),
            dma((2,)),
        ],
        compiler_params=pltpu.CompilerParams(
            collective_id=0, has_side_effects=True, vmem_limit_bytes=60 * 1024 * 1024
        ),
        name="forward",
    )(lengths, bias_table, routes_t, tokens, cotangent, gains, router, attn_qkv, attn_out, expert_in, expert_out)


def expert_kernel(
    grps,
    exps,
    cap,
    deal,
    routes_t,
    comb,
    n_all,
    cot_all,
    both_w,
    down_w,
    in_low,
    down_slab,
    h1,
    n_total,
    y_half,
    y_far,
    c_in,
    both_g,
    down_g,
    in_parts,
    down_parts,
    place,
    marks,
    n_rows,
    g_rows,
    both_v,
    down_v,
    raw_n,
    raw_g,
    y_acc,
    n_acc,
    both_d,
    active,
    n_bufs,
    c_sum,
    out_y,
    load_sem,
    raw_sem,
    out_sem,
    in_sem,
    in_down_sem,
    home_sem,
    home_down_sem,
    stage_sem,
    far_sem,
    n_sem,
    c_sem,
):
    at = Where(grps, exps)
    rows, width = n_all.shape[1:]
    tiles = Tiles(down_slab.shape[0], at.reps)
    size = tiles.size
    slots = exps * cap
    members = QUAD * exps
    loads = [pltpu.make_async_copy(both_w.at[t], both_v.at[t], load_sem.at[0, t]) for t in range(2)] + [
        pltpu.make_async_copy(down_w.at[t], down_v.at[t], load_sem.at[1, t]) for t in range(2)
    ]
    for copy in loads:
        copy.start()

    def raw_copies(q):
        here = pl.ds(pl.multiple_of(q * exps, exps), exps)
        return [
            pltpu.make_async_copy(n_all.at[here], raw_n.at[pl.ds(q % 2 * exps, exps)], raw_sem.at[0, q % 2]),
            pltpu.make_async_copy(cot_all.at[here], raw_g.at[pl.ds(q % 2 * exps, exps)], raw_sem.at[1, q % 2]),
        ]

    for copy in raw_copies(0):
        copy.start()

    beside = at.exp + 1 - 2 * (at.exp % 2)
    greet(*neighbours(at))()
    last = tiles.count - 1
    incoming = Outward(
        at, tiles, last, in_low, down_slab, both_v.at[last], down_v.at[last], None, in_sem, in_down_sem
    )
    incoming.start()
    home = Homeward(
        at, tiles, 0, both_v.at[0], down_v.at[0], in_parts, down_parts, home_sem, home_down_sem, (0,)
    )

    earlier = jnp.where(row_of((rows, rows)) < lane_of((rows, rows)), 1.0, 0.0).astype(low)
    slot = row_of((cap, rows)).astype(full)

    def dispatch(q, _):
        @pl.when(q + 1 < QUAD)
        def _():
            for copy in raw_copies(q + 1):
                copy.start()

        for copy in raw_copies(q):
            copy.wait()
        lines = []
        for j in range(exps):
            seq = at.grp * members + q * exps + j
            pair = routes_t[:, pl.ds(pl.multiple_of(seq * rows, rows), rows)]
            lines.append(jnp.logical_or(pair[0:1] == at.exp, pair[1:2] == at.exp))
        lines = [jnp.where(line, 1.0, 0.0) for line in lines] + [jnp.zeros((8 - exps, rows), full)]
        hot_low = jnp.concatenate(lines, axis=0).astype(low)
        before = dot(hot_low, earlier)
        for j in range(exps):
            s = q * exps + j
            inside = jnp.logical_and(slot == before[j : j + 1, :], hot_low[j : j + 1, :].astype(full) > 0.5)
            here = jnp.where(inside, 1.0, 0.0)
            place[s] = here.astype(low)
            g = raw_g[q % 2 * exps]
            for b in range(1, exps):
                g = jnp.where(deal[at.grp * members + s] == at.grp * members + q * exps + b, raw_g[q % 2 * exps + b], g)
            where = pl.ds(pl.multiple_of(s * cap, cap), cap)
            n_rows[where] = dot(here.astype(low), raw_n[q % 2 * exps + j]).astype(low)
            g_rows[where] = dot(here.astype(low), g).astype(low)
            marks[where, 0:1] = jnp.sum(here * comb[s, pl.ds(at.exp, 1), :], axis=1, keepdims=True)
            marks[where, 1:2] = jnp.zeros((cap, 1), full)
        return 0

    lax.fori_loop(0, QUAD, dispatch, 0)
    for copy in loads:
        copy.wait()
    curve = math.sqrt(2.0 / math.pi)

    core = at.exp % 2

    plane = at.quad * exps + at.exp
    sibling = at.device(at.rep, beside)
    dn = Halving(at, n_bufs, n_sem, [[0, 1, 2], [1, 2, 0], [2, 0, 1]])

    def n_copy(j):
        return send(raw_n.at[j], n_bufs[0].at[j], far_sem.at[0, 0, j], far_sem.at[0, 1, j], sibling)

    def y_copies(j):
        return (
            pltpu.make_async_copy(out_y.at[j % 2], y_half.at[j], out_sem.at[j % 2]),
            send(raw_n.at[j], y_far.at[j], far_sem.at[1, 0, j], far_sem.at[1, 1, j], sibling),
        )

    def c_copy(k):
        other = (plane + k) % members
        return send(
            c_sum.at[other],
            c_in.at[plane],
            c_sem.at[0, other],
            c_sem.at[1, plane],
            (at.grp, other // exps, other % exps),
        )

    def slots_of(s):
        return pl.ds(pl.multiple_of(s * cap, cap), cap)

    def n_rows_of(s):
        where = slots_of(s)
        line = jnp.sum(place[s].astype(full) * marks[where, 1:2], axis=0, keepdims=True)
        c_sum[s] = jnp.broadcast_to(line, (8, rows))
        return tn(place[s], n_acc[where]).astype(low)

    def y_rows_of(p):
        first = p // exps * exps
        spot = at.grp * members + p
        here, y = place[first], y_acc[slots_of(first)]
        for c in range(1, exps):
            taken = deal[at.grp * members + first + c] == spot
            here = jnp.where(taken, place[first + c], here)
            y = jnp.where(taken, y_acc[slots_of(first + c)], y)
        return (tn(here, y) + jnp.where(deal[at.me] == spot, h1[...], 0.0)).astype(low)

    def give_n(j):
        raw_n[j] = n_rows_of(2 * j + 1 - core)
        n_copy(j).start()
        raw_g[j] = n_rows_of(2 * j + core)

    def add_n(quad):
        for k in range(exps // 2):
            j = quad * (exps // 2) + k
            arrived(n_bufs[0].at[j], far_sem.at[0, 1, j])
            n_bufs[0][j] = n_bufs[0][j] + raw_g[j]

    def give_y(j, _):
        @pl.when(j >= 2)
        def _():
            y_copies(j - 2)[0].wait()

        out_y[j % 2] = y_rows_of(2 * j + core)
        n_copy(j).wait_send()
        raw_n[j] = y_rows_of(2 * j + 1 - core)
        for copy in y_copies(j):
            copy.start()
        return 0

    def start_c(k, _):
        c_copy(k).start()
        return 0

    def tile_work(f, _):
        @pl.when(f == last)
        def _():
            incoming.arrive()

        def chunk(i, _):
            c = jnp.where(i == 0, at.near(3), jnp.where(i == 1, at.near(1), jnp.where(i == 2, at.near(2), at.quad)))
            here = pl.ds(pl.multiple_of(c * slots, slots), slots)
            share = marks[here, 0:1]
            both = dot(n_rows[here], both_v[f])
            gate_part, up_part = both[:, :size], both[:, size:]
            grad = nt(g_rows[here], down_v[f])
            square = gate_part * gate_part
            bend = jnp.tanh(curve * gate_part * (1.0 + 0.044715 * square))
            half = 0.5 * (1.0 + bend)
            gelu = gate_part * half
            slope = half + (0.5 * curve) * gate_part * (1.0 - bend * bend) * (1.0 + (3 * 0.044715) * square)
            value = gelu * up_part
            marks[here, 1:2] += jnp.sum(value * grad, axis=1, keepdims=True)
            grad = grad * share
            active[f % 2, here] = (value * share).astype(low)
            both_d[f % 2, here, :size] = (grad * up_part * slope).astype(low)
            both_d[f % 2, here, size:] = (grad * gelu).astype(low)
            y = dot(active[f % 2, here], down_v[f])
            y_acc[here] = jnp.where(f == 0, y, y_acc[here].astype(full) + y).astype(low)
            n_back = nt(both_d[f % 2, here], both_v[f])
            n_acc[here] = jnp.where(f == 0, n_back, n_acc[here].astype(full) + n_back).astype(low)

            @pl.when(f == last)
            def _():
                for k in range(exps // 2):
                    give_n(c * (exps // 2) + k)

            @pl.when(jnp.logical_and(f == last, i == 2))
            def _():
                add_n(at.near(3))

            @pl.when(jnp.logical_and(f == last, i == 3))
            def _():
                add_n(at.near(1))
                dn.start(0, 1)

            return 0

        lax.fori_loop(0, QUAD, chunk, 0)

        @pl.when(f == 0)
        def _():
            weight_work(0)

        return 0

    def weight_work(f):
        def columns(m, _):
            cols = pl.ds(pl.multiple_of(m * (width // 2), width // 2), width // 2)
            both_v[f, cols] = tn(n_rows[:, cols], both_d[f % 2]).astype(low)
            down_v[f, :, cols] = tn(active[f % 2], g_rows[:, cols]).astype(low)
            return 0

        lax.fori_loop(0, 2, columns, 0)

        for copy in stage_copies(f):
            copy.start()
        if f == 0:
            home.start()

    def stage_copies(f):
        copies = [pltpu.make_async_copy(both_v.at[f], both_g.at[f], stage_sem.at[0, f])]
        if f:
            copies.append(pltpu.make_async_copy(down_v.at[f], down_g.at[f - 1], stage_sem.at[1, f]))
        return copies

    lax.fori_loop(0, tiles.count, tile_work, 0)

    half = members // 2
    lax.fori_loop(1, members, start_c, 0)
    c_in[plane] = c_sum[plane]
    weight_work(1)
    add_n(at.near(2))
    dn.start(0, 2)
    add_n(at.quad)
    dn.start(0, 0)
    weight_work(2)
    lax.fori_loop(0, half, give_y, 0)
    for step in range(len(dn.chip_bits)):
        dn.next(step)
    n_total[...] = dn.result()[0]
    for j in (half - 2, half - 1):
        y_copies(j)[0].wait()
    for f in range(tiles.count):
        for copy in stage_copies(f):
            copy.wait()

    def core_in(j, _):
        y_copies(j)[1].wait_send()
        arrived(y_far.at[j], far_sem.at[1, 1, j])
        return 0

    lax.fori_loop(0, half, core_in, 0)

    def c_done(k, _):
        c_copy(k).wait_send()
        other = (plane + k) % members
        arrived(c_in.at[other], c_sem.at[1, other])
        return 0

    lax.fori_loop(1, members, c_done, 0)
    dn.finish()
    home.arrive()
    incoming.sent()
    home.sent()


def expert_call(grps, exps, cap, deal, routes_t, comb_all, n_all, cot_all, both_w, down_w, in_low, down_slab, h1):
    members, rows, width = n_all.shape
    reps = grps * QUAD
    tiles = Tiles(down_slab.shape[0], reps)
    size = tiles.size
    slab, both_hidden = in_low.shape
    units = down_slab.shape[0]
    slots = exps * cap
    chip_bits = bits_of(members) - 1
    shape = jax.ShapeDtypeStruct
    vmem = pl.BlockSpec(memory_space=pltpu.VMEM)
    smem = pl.BlockSpec(memory_space=pltpu.SMEM)
    hbm = pl.BlockSpec(memory_space=pl.ANY)
    results = [
        (shape((rows, width), low), vmem),
        (shape((members // 2, rows, width), low), hbm),
        (shape((members // 2, rows, width), low), hbm),
        (shape((members, 8, rows), full), vmem),
        (shape((tiles.count, width, 2 * size), low), hbm),
        (shape((2, size, width), low), hbm),
        (shape((grps, slab, both_hidden), low), hbm),
        (shape((grps, units, width), low), hbm),
    ]
    dma = pltpu.SemaphoreType.DMA
    return pl.pallas_call(
        functools.partial(expert_kernel, grps, exps, cap),
        out_shape=[r[0] for r in results],
        in_specs=[smem] + [vmem] * 2 + [hbm] * 6 + [vmem],
        out_specs=[r[1] for r in results],
        scratch_shapes=[
            pltpu.VMEM((members, cap, rows), low),
            pltpu.VMEM((QUAD * slots, 128), full),
            pltpu.VMEM((QUAD * slots, width), low),
            pltpu.VMEM((QUAD * slots, width), low),
            pltpu.VMEM((tiles.count, width, 2 * size), low),
            pltpu.VMEM((tiles.count, size, width), low),
            pltpu.VMEM((2 * exps, rows, width), low),
            pltpu.VMEM((2 * exps, rows, width), low),
            pltpu.VMEM((QUAD * slots, width), low),
            pltpu.VMEM((QUAD * slots, width), low),
            pltpu.VMEM((2, QUAD * slots, 2 * size), low),
            pltpu.VMEM((2, QUAD * slots, size), low),
            [pltpu.VMEM((members >> (1 + step), rows, width), low) for step in range(chip_bits + 1)],
            pltpu.VMEM((members, 8, rows), full),
            pltpu.VMEM((2, rows, width), low),
            dma((2, 2)),
            dma((2, 2)),
            dma((2,)),
            dma((2, 2 * reps)),
            dma((2, reps + 1)),
            dma((2, 2 * reps)),
            dma((2, max(QUAD, grps))),
            dma((2, tiles.count)),
            dma((2, 2, members // 2)),
            dma((2, 3 << chip_bits)),
            dma((2, members)),
        ],
        compiler_params=pltpu.CompilerParams(
            collective_id=2, has_side_effects=True, vmem_limit_bytes=60 * 1024 * 1024
        ),
        name="experts",
    )(deal, routes_t, comb_all, n_all, cot_all, both_w, down_w, in_low, down_slab, h1)


def adamw_root(weight, moment, second, gradient, step_rate, decay_factor):
    new_moment = beta_one * moment + (1.0 - beta_one) * gradient
    new_second = beta_two * second + (1.0 - beta_two) * gradient * gradient
    root = lax.rsqrt(new_second * (1.0 / (1.0 - beta_two**STEP)))
    step = new_moment * (root * (1.0 - eps_adam * root))
    keep = 1.0 - step_rate * decay_factor
    return (new_moment, new_second, keep * weight - (step_rate / (1.0 - beta_one**STEP)) * step)


def adam_kernel(exps, *refs):
    in_parts, down_parts, qkv_grad, out_grad, small = refs[:5]
    states, news, bias_grad = refs[5:26], refs[26:47], refs[47]
    heads = HEADS // exps
    width = small.shape[1]

    def update(i, grad, rate, decay):
        weight, first, second = [state[...] for state in states[3 * i : 3 * i + 3]]
        values = adamw_root(weight, first, second, grad, rate, decay)
        for new, value in zip(news[3 * i : 3 * i + 3], values, strict=True):
            new[...] = value

    def total(parts):
        result = parts[0].astype(full)
        for k in range(1, parts.shape[0]):
            result = result + parts[k].astype(full)
        return result

    @pl.when(pl.program_id(0) == 0)
    def _():
        update(0, qkv_grad[...], 1.5 / math.sqrt(D), 0.1)
        update(1, out_grad[...], 6.0 / math.sqrt(D), 0.1)
        for e in range(exps):
            for h in range(heads):
                bias_grad[e * heads + h : e * heads + h + 1, :] = small[
                    exps + 3 + e : exps + 4 + e, h * 128 : h * 128 + BUCKETS
                ]
        update(2, bias_grad[...], 0.3, 0.0)
        update(3, small[0:exps, :], 1.0 / math.sqrt(D), 0.1)
        update(4, small[exps : exps + 2, :], 0.5, 0.0)

    update(5, total(in_parts), 1.5 / math.sqrt(D), 0.1)
    update(6, total(down_parts), 1.5 / math.sqrt(FF), 0.1)


def adam_call(exps, in_parts, down_parts, qkv_grad, out_grad, small, states):
    steps = 4

    def whole(array):
        return pl.BlockSpec(array.shape, lambda i: (0,) * array.ndim)

    def columns(array):
        block = array.shape[:-1] + (array.shape[-1] // steps,)
        return pl.BlockSpec(block, lambda i: (0,) * (array.ndim - 1) + (i,))

    specs = [whole(state) for state in states[:15]]
    specs += [columns(state) for state in states[15:18]] + [columns(state) for state in states[18:]]
    return pl.pallas_call(
        functools.partial(adam_kernel, exps),
        grid=(steps,),
        in_specs=[columns(in_parts), columns(down_parts), whole(qkv_grad), whole(out_grad), whole(small)] + specs,
        out_specs=specs,
        out_shape=[jax.ShapeDtypeStruct(state.shape, full) for state in states],
        scratch_shapes=[pltpu.VMEM((HEADS, BUCKETS), full)],
        compiler_params=pltpu.CompilerParams(vmem_limit_bytes=60 * 1024 * 1024),
        name="adam",
    )(in_parts, down_parts, qkv_grad, out_grad, small, *states)


def backward_kernel(
    grps,
    exps,
    lengths,
    deal,
    y_half,
    y_far,
    both_g,
    down_g,
    in_before,
    down_before,
    n1_in,
    cot_all,
    routes_t,
    tokens,
    n_total,
    c_in,
    n2_in,
    probs_in,
    h1_from,
    qkv_from,
    pb_from,
    mine_from,
    wqkv_from,
    wout_from,
    gains,
    router_t,
    *rest,
):
    token_grad, block_out, in_parts, down_parts, qkv_grad, out_grad, small_out = rest[:7]
    scratch = rest[7:]
    (
    h1_in,
    qkv,
    pb,
    mine,
    wqkv,
    wout,
    kept,
    y_bufs,
    dh1,
    dz_send,
    dz_all,
    do_send,
    do_in,
    bias_sum,
    dqkv,
    dqkv_t,
    dn1_send,
    dn1_in,
    wq_send,
    og_send,
    mids,
    far_send,
    far_in,
    small_send,
    small_exp,
    small_sum,
    small_rep,
    y_sem,
    load_sem,
    weight_sem,
    down_sem,
    dz_sem,
    do_sem,
    dn1_sem,
    wq_sem,
    og_sem,
    mid_sem,
    far_sem,
    small_sem,
    small2_sem,
    n1_sem,
    operand_sem,
    ) = scratch
    at = Where(grps, exps)
    reps = at.reps
    rows, width = tokens.shape
    heads = HEADS // exps
    head_dim = width // HEADS
    head_cols = heads * head_dim
    block_cols = min(128, head_cols)
    row_block = wqkv.shape[2]
    out_cols = wout.shape[3]
    tiles = Tiles(down_parts.shape[1], reps)
    scale = 1.0 / math.sqrt(head_dim)
    SEND, RECV = 0, 1
    plane = at.quad * exps + at.exp
    members = QUAD * exps

    def exp_peer(k):
        return (at.exp + k) % exps

    router = router_t[...]
    met = greet(*neighbours(at))
    n1 = kept.at[0:exps]
    group = pl.ds(pl.multiple_of(at.quad * exps, exps), exps)
    cot_copy = pltpu.make_async_copy(cot_all.at[group], dn1_send, n1_sem.at[1])
    cot_copy.start()
    loads = [
        pltpu.make_async_copy(src, dst, operand_sem.at[i])
        for i, (src, dst) in enumerate(
            ((h1_from, h1_in), (wout_from, wout), (qkv_from, qkv), (pb_from, pb), (mine_from, mine), (wqkv_from, wqkv))
        )
    ]
    ys = Halving(at, y_bufs, y_sem, [[0, 1, 2], [0, 1, 2], [1, 0, 2]])
    half_loads = [
        pltpu.make_async_copy(y_far, y_bufs[0], load_sem.at[0]),
        pltpu.make_async_copy(y_half, kept, load_sem.at[1]),
    ]
    for copy in loads + half_loads:
        copy.start()

    span = 2 * rows
    met()

    homes = [
        Homeward(
            at,
            tiles,
            t,
            both_g.at[t],
            down_g.at[t - 1] if t else None,
            in_parts,
            down_parts,
            weight_sem.at[t],
            down_sem.at[t],
            (0, 1) if t else (1,),
        )
        for t in range(tiles.count)
    ]
    homes[0].start()
    homes[1].start()
    n1_copy = pltpu.make_async_copy(n1_in, n1, n1_sem.at[0])

    lane = lane_of((rows, 128))
    comb_rows = []
    for e in range(exps):
        total = c_in[e]
        for q in range(1, QUAD):
            total = total + c_in[q * exps + e]
        comb_rows.append(total[0:1, :])
    comb_rows.append(jnp.zeros((128 - exps, rows), full))
    comb_grad = jnp.concatenate(comb_rows, axis=0).T
    valid = row_of((rows, 1)) < lengths[at.me]
    probs = probs_in[...]
    hot = routed(routes_t, at.me, rows)
    picked = jnp.where(hot, probs, 0.0)
    total = jnp.sum(picked, axis=1, keepdims=True)
    gate = picked / total
    gate_grad_rows = jnp.where(valid, comb_grad, 0.0)
    spread_grad = jnp.sum(gate_grad_rows * gate, axis=1, keepdims=True)
    probs_grad = jnp.where(hot, (gate_grad_rows - spread_grad) / total, 0.0)
    logit_grad = probs * (probs_grad - jnp.sum(probs_grad * probs, axis=1, keepdims=True))
    small_rows = small_send.shape[0]
    small_send[...] = jnp.zeros_like(small_send)
    router_back = jnp.dot(
        logit_grad, jnp.concatenate([router, jnp.zeros((128 - exps, width), full)], axis=0),
        precision=highest, preferred_element_type=full,
    )
    for copy in loads:
        copy.wait()
    h1 = h1_in[...]
    r2 = lax.rsqrt(jnp.mean(h1 * h1, axis=1, keepdims=True) + eps_norm)

    steps = len(ys.chip_bits)
    n2_grad = router_back + n_total[...].astype(full)
    scaled = n2_grad * gains[1:2, :]
    cot_copy.wait()
    dealt = deal[at.me] - at.base
    g = dn1_send[0]
    for e in range(1, exps):
        g = jnp.where(dealt == e, dn1_send[e], g)
    hidden_grad = (
        jnp.where(valid, g.astype(full), 0.0)
        + r2 * scaled
        - h1 * (r2 * r2 * r2) * jnp.mean(scaled * h1, axis=1, keepdims=True)
    )
    dh1[...] = hidden_grad
    small_send[exps + 1 : exps + 2, :] = jnp.sum(n2_grad * h1 * r2, axis=0, keepdims=True)
    branch = hidden_grad.astype(low)
    dz_send[...] = branch
    for e in range(exps):
        total = jnp.zeros((rows, row_block), full)
        for r in range(reps):
            total = total + nt(branch[:, r * out_cols : (r + 1) * out_cols], wout[e, r])
        do_send[e] = total.astype(low)

    def do_copies():
        return [
            send(
                do_send.at[exp_peer(k)],
                do_in.at[at.exp],
                do_sem.at[SEND, exp_peer(k)],
                do_sem.at[RECV, at.exp],
                at.device(at.rep, exp_peer(k)),
            )
            for k in range(1, exps)
        ]

    for copy in do_copies():
        copy.start()
    pltpu.make_async_copy(do_send.at[at.exp], do_in.at[at.exp], do_sem.at[RECV, at.exp]).start()

    group_dz = Group(at, dz_send, dz_all, dz_sem)
    dz_all[at.exp] = branch
    for copy in half_loads:
        copy.wait()

    def add_halves(j, _):
        y_bufs[0][j] = y_bufs[0][j] + kept[j]
        return 0

    lax.fori_loop(0, kept.shape[0], add_halves, 0)
    n1_copy.start()

    bias_sum[...] = jnp.zeros_like(bias_sum)

    def dn1_copies():
        beside, across = turn(at.exp, 2), turn(at.exp, 1)
        return [
            functools.partial(
                send, dn1_send.at[k], dn1_in.at[j], dn1_sem.at[SEND, j], dn1_sem.at[RECV, j], at.device(at.rep, to)
            )
            for k, j, to in ((turn(at.exp, 0), 2, beside), (across, 0, across), (beside, 1, beside))
        ]

    def attend_back(i, _):
        s = turn(at.exp, i)
        arrived(do_in.at[s], do_sem.at[RECV, s])

        @pl.when(i == 0)
        def _():
            group_dz.start()
            ys.start(0)

        @pl.when(i == 1)
        def _():
            homes[2].start()

        @pl.when(i == 2)
        def _():
            group_dz.pass_on()

        block_lane = lane_of((rows, block_cols))
        for c in range(head_cols // block_cols):
            cols = slice(c * block_cols, (c + 1) * block_cols)
            k_cols = slice(head_cols + c * block_cols, head_cols + (c + 1) * block_cols)
            v_cols = slice(2 * head_cols + c * block_cols, 2 * head_cols + (c + 1) * block_cols)
            q = qkv[s, :, cols] * scale
            k = qkv[s, :, k_cols]
            v = qkv[s, :, v_cols]
            do = do_in[s, :, cols]
            dq = jnp.zeros((rows, block_cols), full)
            dk = jnp.zeros((rows, block_cols), full)
            dv = jnp.zeros((rows, block_cols), full)
            for t in range(block_cols // head_dim):
                h = c * (block_cols // head_dim) + t
                here = jnp.logical_and(block_lane >= t * head_dim, block_lane < (t + 1) * head_dim)
                zero = jnp.zeros_like(q)
                do_h = jnp.where(here, do, zero)
                weights = pb[s * heads + h]
                p = weights.astype(full)
                dp = nt(do_h, v)
                delta = jnp.sum(dp * p, axis=1, keepdims=True)
                ds = (p * (dp - delta)).astype(low)
                bias_sum[h] += ds.astype(full)
                dv = jnp.where(here, tn(weights, do), dv)
                dq = jnp.where(here, jnp.dot(ds, k, preferred_element_type=full), dq)
                dk = jnp.where(here, tn(ds, q), dk)
            dqkv[:, cols] = (dq * scale).astype(low)
            dqkv[:, k_cols] = dk.astype(low)
            dqkv[:, v_cols] = dv.astype(low)
        dqkv_t[:, pl.ds(pl.multiple_of(s * rows, rows), rows)] = dqkv[...].T
        for e in range(exps):
            dn1_send[s, :, e * row_block : (e + 1) * row_block] = jnp.dot(
                dqkv[...], wqkv[e], preferred_element_type=full
            ).astype(low)

        @pl.when(i == 0)
        def _():
            dn1_copies()[0]().start()

        @pl.when(i == 1)
        def _():
            arrived(dn1_in.at[2], dn1_sem.at[RECV, 2])
            dn1_send[s] = (dn1_send[s].astype(full) + dn1_in[2].astype(full)).astype(low)
            dn1_copies()[1]().start()

        @pl.when(i == 2)
        def _():
            dn1_copies()[2]().start()

        return 0

    lax.fori_loop(0, exps, attend_back, 0)

    n1_copy.wait()
    seg = wq_send.shape[2]
    parts = wq_send.shape[1]
    segs = mids.shape[1] - 1
    for e in range(exps):
        part = kept[0:exps, :, e * row_block : (e + 1) * row_block].reshape(exps * rows, row_block)
        total = dot(dqkv_t[...], part)
        for j in range(parts):
            wq_send[e, j] = total[j * seg : (j + 1) * seg].astype(low)

    def owner(j):
        section, within = j // (head_cols // seg), j % (head_cols // seg)
        col = section * width + at.exp * head_cols + within * seg
        block = col // seg
        return block // segs, block % segs

    def mid_place(grp, k, quad):
        return (grp * (segs + 1) + k) * QUAD + quad

    def mid_copy(src, send_sem, rep, k, e):
        dst = mids.at[rep // QUAD, k, at.quad]
        recv = mid_sem.at[mid_place(rep // QUAD, k, at.quad)]
        stays = jnp.logical_and(rep % QUAD == at.quad, e == at.exp)
        return (
            stays,
            functools.partial(send, src, dst, send_sem, recv, (at.grp, rep % QUAD, e)),
            functools.partial(pltpu.make_async_copy, src, dst, recv),
        )

    def wq_copy(i):
        e, j = i // parts, i % parts
        rep, k = owner(j)
        return mid_copy(wq_send.at[e, j], wq_sem.at[i], rep, k, e)

    def og_copy(r):
        return mid_copy(og_send.at[r], og_sem.at[r], r, segs, at.exp)

    def go(copies, act, act_local):
        stays, away, local = copies

        @pl.when(jnp.logical_not(stays))
        def _():
            act(away)

        if act_local:

            @pl.when(stays)
            def _():
                act_local(local)

    def over(count, copies, act, act_local):
        def one(i, _):
            go(copies(i), act, act_local)
            return 0

        lax.fori_loop(0, count, one, 0)

    over(exps * parts, wq_copy, lambda copy: copy().start(), lambda copy: copy().start())
    group_dz.arrive()
    grad = tn(mine[...].reshape(exps * rows, head_cols), dz_all[...].reshape(exps * rows, width))
    for r in range(reps):
        og_send[r] = grad[:, r * out_cols : (r + 1) * out_cols].T.astype(low)
    over(reps, og_copy, lambda copy: copy().start(), lambda copy: copy().start())

    n1_grad = dn1_send[at.exp].astype(full)
    for j in range(2):
        arrived(dn1_in.at[j], dn1_sem.at[RECV, j])
        n1_grad = n1_grad + dn1_in[j].astype(full)
    x = tokens[...].astype(full)
    r1 = lax.rsqrt(jnp.mean(x * x, axis=1, keepdims=True) + eps_norm)
    scaled = n1_grad * gains[0:1, :]
    token_grad[...] = (
        dh1[...] + r1 * scaled - x * (r1 * r1 * r1) * jnp.mean(scaled * x, axis=1, keepdims=True)
    )
    small_send[exps : exps + 1, :] = jnp.sum(n1_grad * x * r1, axis=0, keepdims=True)

    router_rows = lax.dot_general(
        logit_grad, n2_in[...].astype(full), (((0,), (0,)), ((), ())), preferred_element_type=full, precision=highest
    )
    small_send[0:exps, :] = router_rows[0:exps, :]

    line_lane = lane_of((8, 128))
    line_row = row_of((8, 128))
    bias_line = jnp.zeros((8, 128), full)
    flip = jnp.where(row_of((rows, rows)) + lane_of((rows, rows)) == rows - 1, 1.0, 0.0).astype(low)
    turned_bucket = bucket_of(rows - 1 - lane_of((8, span)))
    for h in range(heads):
        high = bias_sum[h].astype(low)
        rest = (bias_sum[h] - high.astype(full)).astype(low)
        flipped = dot(high, flip) + dot(rest, flip)
        square = jnp.concatenate([flipped, jnp.zeros((rows, rows), full)], axis=1)
        turned = pltpu.roll(square, 0, 1, stride=1, stride_axis=0)
        sums = jnp.broadcast_to(jnp.sum(turned, axis=0, keepdims=True), (8, span))
        for b in range(BUCKETS):
            value = jnp.sum(jnp.where(turned_bucket == b, sums, 0.0), axis=1, keepdims=True)
            bias_line = jnp.where(jnp.logical_and(line_row == h, line_lane == b), value, bias_line)
    for h in range(heads):
        small_send[exps + 2 : exps + 3, h * 128 : (h + 1) * 128] = bias_line[h : h + 1, :]

    def small_copies():
        return [
            send(
                small_send,
                small_exp.at[at.exp],
                small_sem.at[SEND, exp_peer(k)],
                small_sem.at[RECV, at.exp],
                at.device(at.rep, exp_peer(k)),
            )
            for k in range(1, exps)
        ]

    for copy in small_copies():
        copy.start()
    small_exp[at.exp] = small_send[...]
    ys.next(0)

    def mid_sum(grp, k):
        for q in range(QUAD):
            arrived(mids.at[grp, k, q], mid_sem.at[mid_place(grp, k, q)])
        total = mids[grp, k, 0].astype(full)
        for q in range(1, QUAD):
            total = total + mids[grp, k, q].astype(full)
        return total

    far = 1 - at.grp
    for k in range(segs + 1):
        far_send[k] = mid_sum(far, k).astype(low)

    def far_copy():
        return send(far_send, far_in, far_sem.at[SEND], far_sem.at[RECV], (far, at.quad, at.exp))

    far_copy().start()
    ys.next(1)
    for k in range(1, exps):
        arrived(small_exp.at[exp_peer(k)], small_sem.at[RECV, exp_peer(k)])
    total = small_exp[0]
    for e in range(1, exps):
        total = total + small_exp[e]
    small_sum[0] = total
    for e in range(exps):
        small_sum[0, exps + 3 + e : exps + 4 + e, :] = small_exp[e, exps + 2 : exps + 3, :]

    def small2_copies():
        return [
            send(
                small_sum.at[0],
                small_rep.at[at.rep],
                small2_sem.at[SEND, (at.rep + k) % reps],
                small2_sem.at[RECV, at.rep],
                at.device((at.rep + k) % reps, at.exp),
            )
            for k in range(1, reps)
        ]

    for copy in small2_copies():
        copy.start()
    small_rep[at.rep] = small_sum[0]
    for step in range(2, steps):
        ys.next(step)
    length = lengths[at.base]
    for e in range(1, exps):
        length = jnp.where(deal[at.base + e] == at.me, lengths[at.base + e], length)
    block = ys.result()[0]
    block_out[...] = jnp.where(row_of((rows, 1)) < length, block, jnp.zeros_like(block))
    for k in range(1, reps):
        arrived(small_rep.at[(at.rep + k) % reps], small2_sem.at[RECV, (at.rep + k) % reps])
    total = small_rep[0]
    for r in range(1, reps):
        total = total + small_rep[r]
    small_out[...] = total

    near = [mid_sum(at.grp, k) for k in range(segs + 1)]
    arrived(far_in, far_sem.at[RECV])
    grads = [(near[k] + far_in[k].astype(full)).T for k in range(segs + 1)]
    qkv_grad[...] = jnp.concatenate(grads[:segs], axis=1)
    out_grad[...] = grads[segs]
    for home in homes:
        home.arrive()

    ys.finish()

    for home in homes:
        home.sent()

    over(exps * parts, wq_copy, lambda copy: copy().wait_send(), None)
    over(reps, og_copy, lambda copy: copy().wait_send(), None)
    far_copy().wait_send()
    for copies in (do_copies(), small_copies(), small2_copies()):
        for copy in copies:
            copy.wait_send()
    for copy in dn1_copies():
        copy().wait_send()
    group_dz.sent()


def routed(routes_t, seq, rows):
    pair = routes_t[:, pl.ds(pl.multiple_of(seq * rows, rows), rows)].astype(full)
    cols = jnp.concatenate([pair, jnp.zeros((126, rows), full)], axis=0).T
    lane = lane_of((rows, 128)).astype(full)
    return jnp.logical_or(lane == cols[:, 0:1], lane == cols[:, 1:2])


def backward_call(
    grps, exps, lengths, deal, y_half, y_far, both_g, down_g, in_before, down_before, n1,
    cot_all, routes_t, tokens, n_total, c_in, n2, probs, h1, qkv, pb, mine, wqkv, wout, gains, router
):
    reps = grps * QUAD
    rows, width = tokens.shape
    heads = HEADS // exps
    head_cols = width // exps
    row_block = wqkv.shape[2]
    out_cols = wout.shape[3]
    shard_cols = 3 * width // reps
    seg = math.gcd(shard_cols, head_cols)
    segs = shard_cols // seg
    parts = 3 * head_cols // seg
    members = QUAD * exps
    chip_bits = bits_of(members) - 1
    small_rows = -(-(2 * exps + 3) // 8) * 8
    shape = jax.ShapeDtypeStruct
    vmem = pl.BlockSpec(memory_space=pltpu.VMEM)
    smem = pl.BlockSpec(memory_space=pltpu.SMEM)
    hbm = pl.BlockSpec(memory_space=pl.ANY)
    results = [
        (shape((rows, width), full), vmem),
        (shape((rows, width), low), vmem),
        (shape(in_before.shape, low), hbm),
        (shape(down_before.shape, low), hbm),
        (shape((row_block, shard_cols), full), vmem),
        (shape((row_block, out_cols), full), vmem),
        (shape((small_rows, width), full), vmem),
    ]
    dma = pltpu.SemaphoreType.DMA
    bufs = [pltpu.VMEM((1 << (chip_bits - s), rows, width), low) for s in range(chip_bits + 1)]
    return pl.pallas_call(
        functools.partial(backward_kernel, grps, exps),
        out_shape=[r[0] for r in results],
        in_specs=[smem] * 2 + [hbm] * 8 + [vmem] * 6 + [hbm] * 6 + [vmem] * 2,
        out_specs=[r[1] for r in results],
        scratch_shapes=[
            pltpu.VMEM(h1.shape, full),
            pltpu.VMEM(qkv.shape, low),
            pltpu.VMEM(pb.shape, low),
            pltpu.VMEM(mine.shape, low),
            pltpu.VMEM(wqkv.shape, low),
            pltpu.VMEM(wout.shape, low),
            pltpu.VMEM((members // 2, rows, width), low),
            list(bufs),
            pltpu.VMEM((rows, width), full),
            pltpu.VMEM((rows, width), low),
            pltpu.VMEM((exps, rows, width), low),
            pltpu.VMEM((exps, rows, head_cols), low),
            pltpu.VMEM((exps, rows, head_cols), low),
            pltpu.VMEM((heads, rows, rows), full),
            pltpu.VMEM((rows, 3 * head_cols), low),
            pltpu.VMEM((3 * head_cols, exps * rows), low),
            pltpu.VMEM((exps, rows, width), low),
            pltpu.VMEM((3, rows, width), low),
            pltpu.VMEM((exps, parts, seg, row_block), low),
            pltpu.VMEM((reps, seg, row_block), low),
            pltpu.VMEM((grps, segs + 1, QUAD, seg, row_block), low),
            pltpu.VMEM((segs + 1, seg, row_block), low),
            pltpu.VMEM((segs + 1, seg, row_block), low),
            pltpu.VMEM((small_rows, width), full),
            pltpu.VMEM((exps, small_rows, width), full),
            pltpu.VMEM((1, small_rows, width), full),
            pltpu.VMEM((reps, small_rows, width), full),
            dma((2, 3 << chip_bits)),
            dma((2,)),
            dma((3, 2, 2 * reps)),
            dma((3, 2, max(QUAD, grps))),
            dma((2, exps)),
            dma((2, exps)),
            dma((2, exps)),
            dma((exps * parts,)),
            dma((reps,)),
            dma((grps * (segs + 1) * QUAD,)),
            dma((2,)),
            dma((2, exps)),
            dma((2, reps)),
            dma((2,)),
            dma((6,)),
        ],
        compiler_params=pltpu.CompilerParams(
            collective_id=1, has_side_effects=True, vmem_limit_bytes=60 * 1024 * 1024
        ),
        input_output_aliases={6: 2, 7: 3},
        name="backward",
    )(
        lengths, deal, y_half, y_far, both_g, down_g, in_before, down_before, n1, cot_all,
        routes_t, tokens, n_total, c_in, n2, probs, h1, qkv, pb, mine, wqkv, wout, gains, router
    )


def per_device(
    tokens,
    cotangent,
    seq_lengths,
    deal,
    routes,
    attn_qkv,
    qkv_first,
    qkv_second,
    attn_out,
    out_first,
    out_second,
    rel_bias,
    bias_first,
    bias_second,
    router,
    router_first,
    router_second,
    norm_gains,
    gains_first,
    gains_second,
    expert_in,
    in_first,
    in_second,
    expert_out,
    down_first,
    down_second,
):
    rows, width = tokens.shape
    experts = router.shape[1]
    capacity = (10 * rows + 4 * experts - 1) // (4 * experts)
    exps = lax.axis_size("exp")
    grps = lax.axis_size("grp")
    routes_t = routes.T
    bias_table = rel_bias.T
    (
        both_w, down_w, cot_all, n_all, comb_all, qkv, pb, context_mine, normed_group, wqkv, wout, hidden_one,
        normed_two, router_probs, in_low, down_low,
    ) = forward_call(
        grps, exps, seq_lengths, bias_table, routes_t, tokens, cotangent, norm_gains.T, router.T,
        attn_qkv, attn_out, expert_in[0], expert_out[0],
    )
    n_total, y_half, y_far, c_in, both_g, down_g, in_before, down_before = expert_call(
        grps, exps, capacity, deal, routes_t, comb_all, n_all, cot_all, both_w, down_w, in_low, down_low,
        hidden_one,
    )
    token_grad, block_out, in_parts, down_parts, qkv_grad, out_grad, small = backward_call(
        grps, exps, seq_lengths, deal, y_half, y_far, both_g, down_g,
        in_before, down_before, normed_group, cot_all, routes_t, tokens, n_total, c_in, normed_two, router_probs, hidden_one, qkv, pb, context_mine, wqkv,
        wout, norm_gains.T, router.T,
    )
    states = [
        attn_qkv, qkv_first, qkv_second, attn_out, out_first, out_second, bias_table, bias_first.T, bias_second.T,
        router.T, router_first.T, router_second.T, norm_gains.T, gains_first.T, gains_second.T,
        expert_in[0], in_first[0], in_second[0], expert_out[0], down_first[0], down_second[0],
    ]
    new = list(adam_call(exps, in_parts, down_parts, qkv_grad, out_grad, small, states))
    new = new[:6] + [array.T for array in new[6:15]] + [array[None] for array in new[15:]]
    return (block_out, token_grad, *new)


def bucket_onehot(length):
    places = jnp.arange(length, dtype=jnp.int32)
    offset = places[None, :] - places[:, None]
    distance = jnp.abs(offset)
    bucket = 16 * (offset > 0).astype(jnp.int32)
    for threshold in thresholds:
        bucket = bucket + (distance >= threshold).astype(jnp.int32)
    return (bucket[:, :, None] == jnp.arange(BUCKETS, dtype=jnp.int32)[None, None, :]).astype(full)


def swap(pieces, axes):
    return lax.all_to_all(pieces, axes, split_axis=0, concat_axis=0, tiled=True)


def spread(block, axes):
    members = lax.axis_size(axes)
    return swap(jnp.broadcast_to(block[None], (members,) + block.shape), axes)


def plain_device(
    tokens,
    cotangent,
    seq_lengths,
    deal,
    routes,
    attn_qkv,
    qkv_first,
    qkv_second,
    attn_out,
    out_first,
    out_second,
    rel_bias,
    bias_first,
    bias_second,
    router,
    router_first,
    router_second,
    norm_gains,
    gains_first,
    gains_second,
    expert_in,
    in_first,
    in_second,
    expert_out,
    down_first,
    down_second,
):
    rows, width = tokens.shape
    head_dim = width // HEADS
    score_scale = 1.0 / math.sqrt(head_dim)
    experts = router.shape[1]
    capacity = (10 * rows + 4 * experts - 1) // (4 * experts)
    exps = lax.axis_size("exp")
    grps = lax.axis_size("grp")
    reps = grps * QUAD
    heads = HEADS // exps
    head_cols = heads * head_dim
    place = lax.axis_index("exp")
    base = lax.axis_index(REP) * exps
    me = base + place
    slab = expert_in.shape[1]
    units = expert_out.shape[1]
    quarter = grps * units

    row_block = attn_qkv.shape[0]
    qkv_rows = lax.all_gather(attn_qkv.astype(low), REP, axis=1, tiled=True)
    out_rows = lax.all_gather(attn_out.astype(low), REP, axis=1, tiled=True)
    qkv_pieces = jnp.transpose(
        qkv_rows.reshape(row_block, 3, exps, head_cols), (2, 0, 1, 3)
    ).reshape(exps, row_block, 3 * head_cols)
    qkv_mine = swap(qkv_pieces, "exp").reshape(width, 3 * head_cols)
    full_out = spread(out_rows, "exp").reshape(width, width)

    group_tokens = spread(tokens, "exp")
    group_cotangent = spread(cotangent, "exp")
    my_cotangent = lax.dynamic_index_in_dim(group_cotangent, deal[me] - base, 0, keepdims=False)

    my_routes = lax.dynamic_slice_in_dim(routes, me * rows, rows, 0)
    places = jnp.arange(rows, dtype=jnp.int32)
    valid_rows = (places < seq_lengths[me]).astype(full)
    group_lengths = lax.dynamic_slice_in_dim(seq_lengths, base, exps, 0)
    key_ok = places[None, :] < group_lengths[:, None]
    gain_one = norm_gains[:, 0]
    gain_two = norm_gains[:, 1]

    chosen = (my_routes[:, :, None] == jnp.arange(experts, dtype=jnp.int32)[None, None, :]).astype(full)
    flat_routes = my_routes.reshape(-1)
    route_hot = (flat_routes[:, None] == jnp.arange(experts, dtype=jnp.int32)[None, :]).astype(jnp.int32)
    before = jnp.cumsum(route_hot, axis=0) - route_hot
    slot_index = jnp.sum(before * route_hot, axis=-1)
    target = (flat_routes * capacity + slot_index).reshape(rows, 2)
    slots = experts * capacity
    slot_ids = jnp.arange(slots, dtype=jnp.int32)
    place_first = slot_ids[:, None] == target[None, :, 0]
    place_second = slot_ids[:, None] == target[None, :, 1]
    place_any = jnp.logical_or(place_first, place_second).astype(low)

    shard_in = expert_in[0].astype(low).reshape(slab, 2, grps, QUAD, units)
    in_pieces = jnp.transpose(shard_in, (1, 3, 0, 2, 4)).reshape(2, 1, QUAD, slab, quarter)
    in_pieces = jnp.broadcast_to(in_pieces, (2, grps, QUAD, slab, quarter)).reshape(
        2, reps, slab, quarter
    )
    down_mine = spread(expert_out[0].astype(low), "grp").reshape(quarter, width)
    gate_mine = swap(in_pieces[0], REP).reshape(width, quarter)
    up_mine = swap(in_pieces[1], REP).reshape(width, quarter)

    upstream = my_cotangent.astype(full) * valid_rows[:, None]

    def to_experts(block):
        sent = block.reshape((1, experts) + block.shape[1:])
        sent = jnp.broadcast_to(sent, (QUAD,) + sent.shape[1:])
        return swap(sent.reshape((QUAD * experts,) + block.shape[1:]), PLANE)

    def dispatch(values):
        return dot(place_any, values).astype(low).reshape(experts, capacity, width)

    expert_upstream = to_experts(dispatch(upstream.astype(low))).reshape(-1, width)
    active_grad_bare = lax.dot_general(
        expert_upstream, down_mine, (((1,), (1,)), ((), ())), preferred_element_type=full
    )

    x_group = group_tokens.astype(full)
    scale_group = lax.rsqrt(jnp.mean(x_group * x_group, axis=-1, keepdims=True) + eps_norm)
    normed_group = (x_group * scale_group * gain_one).astype(low).reshape(exps * rows, width)
    qkv = dot(normed_group, qkv_mine).astype(low).reshape(exps, rows, 3, heads, head_dim)
    queries = qkv[:, :, 0]
    key_rows = qkv[:, :, 1]
    values = qkv[:, :, 2]
    onehot = bucket_onehot(rows)
    bias_mine = lax.dynamic_slice_in_dim(rel_bias, place * heads, heads, 1)
    bias_table = jnp.einsum("ijb,bh->hij", onehot, bias_mine, precision=highest)

    def scores_of():
        raw = (
            jnp.einsum("sihd,sjhd->shij", queries, key_rows, preferred_element_type=full)
            * score_scale
            + bias_table[None]
        )
        return jnp.where(key_ok[:, None, None, :], raw, -1e30)

    scores = scores_of()
    row_max = jnp.max(scores, axis=-1, keepdims=True)
    log_total = row_max + jnp.log(jnp.sum(jnp.exp(scores - row_max), axis=-1, keepdims=True))
    weights_low = jnp.exp(scores - log_total).astype(low)
    context_mine = (
        jnp.einsum("shij,sjhd->sihd", weights_low, values, preferred_element_type=full)
        .astype(low)
        .reshape(exps, rows, head_cols)
    )
    context = jnp.transpose(swap(context_mine, "exp"), (1, 0, 2)).reshape(rows, width)

    x_float = tokens.astype(full)
    scale_one = lax.rsqrt(jnp.mean(x_float * x_float, axis=-1, keepdims=True) + eps_norm)
    hidden_one = x_float + dot(context, full_out)
    scale_two = lax.rsqrt(jnp.mean(hidden_one * hidden_one, axis=-1, keepdims=True) + eps_norm)
    normed_two = (hidden_one * scale_two * gain_two).astype(low)
    normed_float = normed_two.astype(full)
    router_probs = jax.nn.softmax(jnp.dot(normed_float, router, precision=highest), axis=-1)
    picked = jnp.sum(router_probs[:, None, :] * chosen, axis=-1)
    gate_total = jnp.sum(picked, axis=-1, keepdims=True)
    gate_value = picked / gate_total
    combine = gate_value * valid_rows[:, None]
    combine_slots = jnp.sum(
        jnp.where(place_first, combine[None, :, 0], 0.0)
        + jnp.where(place_second, combine[None, :, 1], 0.0),
        axis=1,
    ).reshape(experts, 1, capacity)

    expert_rows = to_experts(dispatch(normed_two)).reshape(-1, width)
    expert_combine = to_experts(combine_slots).reshape(-1, 1)

    gate_part = dot(expert_rows, gate_mine)
    up_part = dot(expert_rows, up_mine)
    active_float, active_pull = jax.vjp(gated_unit, gate_part, up_part)
    active = active_float.astype(low)
    active_scaled = (active_float * expert_combine).astype(low)
    combine_grad_part = jnp.sum(active_float * active_grad_bare, axis=-1).reshape(
        QUAD * experts, 1, capacity
    )
    gate_part_grad, up_part_grad = active_pull(active_grad_bare * expert_combine)
    gate_part_grad = gate_part_grad.astype(low)
    up_part_grad = up_part_grad.astype(low)
    rows_grad_part = (
        lax.dot_general(gate_part_grad, gate_mine, (((1,), (1,)), ((), ())), preferred_element_type=full)
        + lax.dot_general(up_part_grad, up_mine, (((1,), (1,)), ((), ())), preferred_element_type=full)
    ).astype(low)
    output_part = dot(active, down_mine).astype(low)

    combine_grad_back = swap(combine_grad_part, PLANE)
    rows_grad_back = swap(rows_grad_part.reshape(QUAD * experts, capacity, width), PLANE)
    output_back = swap(output_part.reshape(QUAD * experts, capacity, width), PLANE)

    def transposed_dot(a, b):
        return lax.dot_general(a, b, (((0,), (0,)), ((), ())), preferred_element_type=full)

    down_grad = transposed_dot(active_scaled, expert_upstream).astype(low)
    gate_grad = transposed_dot(expert_rows, gate_part_grad).astype(low)
    up_grad = transposed_dot(expert_rows, up_part_grad).astype(low)
    down_share = jnp.sum(
        swap(down_grad.reshape(grps, units, width), "grp").astype(full), axis=0
    )[None]

    def in_columns(grad):
        back = swap(grad.reshape(reps, slab, quarter), REP).astype(full)
        back = jnp.sum(back.reshape(grps, QUAD, slab, grps, units), axis=0)
        return jnp.transpose(back, (1, 2, 0, 3)).reshape(slab, grps * QUAD * units)

    in_share = jnp.concatenate([in_columns(gate_grad), in_columns(up_grad)], axis=1)[None]

    def from_slots(placed, parts):
        hot = jnp.broadcast_to(placed.astype(low)[None], (QUAD,) + placed.shape).reshape(-1, rows)
        return lax.dot_general(
            hot, parts.reshape(-1, width), (((0,), (0,)), ((), ())), preferred_element_type=full
        )

    mixture = combine[:, :1] * from_slots(place_first, output_back) + combine[:, 1:] * from_slots(
        place_second, output_back
    )
    block_loader = (valid_rows[:, None] * (hidden_one + mixture)).astype(low)
    seq_ids = jnp.arange(deal.shape[0], dtype=jnp.int32)
    dealt_seq = jnp.sum(jnp.where(deal == me, seq_ids, 0))
    block_out = lax.dynamic_index_in_dim(
        spread(block_loader, "exp"), dealt_seq - base, 0, keepdims=False
    )

    combine_grad_slots = jnp.sum(combine_grad_back.reshape(QUAD, slots), axis=0)
    combine_grad = jnp.stack(
        [
            jnp.sum(jnp.where(place_first, combine_grad_slots[:, None], 0.0), axis=0),
            jnp.sum(jnp.where(place_second, combine_grad_slots[:, None], 0.0), axis=0),
        ],
        axis=1,
    )
    gate_grad_value = combine_grad * valid_rows[:, None]
    picked_grad = (
        gate_grad_value - jnp.sum(gate_grad_value * gate_value, axis=-1, keepdims=True)
    ) / gate_total
    probs_grad = jnp.sum(picked_grad[:, :, None] * chosen, axis=1)
    logit_grad = router_probs * (
        probs_grad - jnp.sum(probs_grad * router_probs, axis=-1, keepdims=True)
    )
    router_grad = jnp.dot(normed_float.T, logit_grad, precision=highest)
    normed_grad = jnp.dot(logit_grad, router.T, precision=highest) + from_slots(
        jnp.logical_or(place_first, place_second), rows_grad_back
    )
    scaled_two = normed_grad * gain_two
    hidden_grad = (
        upstream
        + scale_two * scaled_two
        - hidden_one * scale_two**3 * jnp.mean(scaled_two * hidden_one, axis=-1, keepdims=True)
    )
    gain_two_grad = jnp.sum(normed_grad * hidden_one * scale_two, axis=0)
    branch_grad = hidden_grad.astype(low)
    context_grad = lax.dot_general(
        branch_grad, full_out, (((1,), (1,)), ((), ())), preferred_element_type=full
    ).astype(low)
    context_grad_pieces = jnp.transpose(context_grad.reshape(rows, exps, head_cols), (1, 0, 2))
    context_grad_mine = swap(context_grad_pieces, "exp").reshape(exps, rows, heads, head_dim)
    branch_group = spread(branch_grad, "exp").reshape(exps * rows, width)
    out_grad = transposed_dot(context_mine.reshape(exps * rows, head_cols), branch_group).astype(low)

    scores = scores_of()
    probs_again = jnp.exp(scores - log_total)
    weights_again = probs_again.astype(low)
    values_grad = jnp.einsum(
        "shij,sihd->sjhd", weights_again, context_grad_mine, preferred_element_type=full
    )
    probs_grad_att = jnp.einsum(
        "sihd,sjhd->shij", context_grad_mine, values, preferred_element_type=full
    )
    row_delta = jnp.sum(probs_grad_att * probs_again, axis=-1, keepdims=True)
    scores_grad = (probs_again * (probs_grad_att - row_delta)).astype(low)
    scores_grad_sum = jnp.sum(scores_grad.astype(full), axis=0)
    bias_grad_mine = jnp.einsum("hij,ijb->bh", scores_grad_sum, onehot, precision=highest)
    bias_grad = lax.dynamic_update_slice_in_dim(
        jnp.zeros((BUCKETS, HEADS), full), bias_grad_mine, place * heads, 1
    )
    queries_grad = (
        jnp.einsum("shij,sjhd->sihd", scores_grad, key_rows, preferred_element_type=full)
        * score_scale
    )
    keys_grad = (
        jnp.einsum("shij,sihd->sjhd", scores_grad, queries, preferred_element_type=full)
        * score_scale
    )
    qkv_grad = (
        jnp.stack([queries_grad, keys_grad, values_grad], axis=2)
        .astype(low)
        .reshape(exps * rows, 3 * head_cols)
    )
    normed_one_part = lax.dot_general(
        qkv_grad, qkv_mine, (((1,), (1,)), ((), ())), preferred_element_type=full
    ).astype(low)
    normed_one_grad = jnp.sum(
        swap(normed_one_part.reshape(exps, rows, width), "exp").astype(full), axis=0
    )
    scaled_one = normed_one_grad * gain_one
    token_grad = (
        hidden_grad
        + scale_one * scaled_one
        - x_float * scale_one**3 * jnp.mean(scaled_one * x_float, axis=-1, keepdims=True)
    )
    gain_one_grad = jnp.sum(normed_one_grad * x_float * scale_one, axis=0)

    qkv_weight_grad = transposed_dot(normed_group, qkv_grad).astype(low)
    qkv_grad_rows = swap(qkv_weight_grad.reshape(exps, row_block, 3 * head_cols), "exp")
    qkv_grad_rows = jnp.transpose(
        qkv_grad_rows.reshape(exps, row_block, 3, head_cols), (1, 2, 0, 3)
    ).reshape(row_block, reps, -1)
    qkv_share = jnp.sum(
        swap(jnp.transpose(qkv_grad_rows, (1, 0, 2)), REP).astype(full), axis=0
    )
    out_pieces = jnp.transpose(out_grad.reshape(row_block, reps, -1), (1, 0, 2))
    out_share = jnp.sum(swap(out_pieces, REP).astype(full), axis=0)

    small = jnp.concatenate(
        [
            router_grad.reshape(-1),
            jnp.stack([gain_one_grad, gain_two_grad], axis=1).reshape(-1),
            bias_grad.reshape(-1),
        ]
    ).reshape(-1, 128)
    small_total = jnp.sum(lax.all_gather(small, ALL, axis=0, tiled=False), axis=0).reshape(-1)
    router_total = small_total[: router.size].reshape(router.shape)
    gains_total = small_total[router.size : router.size + norm_gains.size].reshape(norm_gains.shape)
    bias_total = small_total[router.size + norm_gains.size :].reshape(rel_bias.shape)

    qkv_new = adamw_update(attn_qkv, qkv_first, qkv_second, qkv_share, 1.5 / math.sqrt(D), 0.1)
    out_new = adamw_update(attn_out, out_first, out_second, out_share, 6.0 / math.sqrt(D), 0.1)
    bias_new = adamw_update(rel_bias, bias_first, bias_second, bias_total, 0.3, 0.0)
    router_new = adamw_update(
        router, router_first, router_second, router_total, 1.0 / math.sqrt(D), 0.1
    )
    gains_new = adamw_update(norm_gains, gains_first, gains_second, gains_total, 0.5, 0.0)
    in_new = adamw_update(expert_in, in_first, in_second, in_share, 1.5 / math.sqrt(D), 0.1)
    down_new = adamw_update(
        expert_out, down_first, down_second, down_share, 1.5 / math.sqrt(FF), 0.1
    )
    return (
        (block_out, token_grad)
        + qkv_new
        + out_new
        + bias_new
        + router_new
        + gains_new
        + in_new
        + down_new
    )


def solution(mesh):
    reps, exps = mesh.devices.shape
    split = Mesh(mesh.devices.reshape(reps // QUAD, QUAD, exps), ALL)
    by_rows = P(ALL, None)
    attn = P("exp", REP)
    expert = P("exp", REP, None)
    return jax.shard_map(
        per_device if (reps, exps) == (2 * QUAD, 4) else plain_device,
        mesh=split,
        in_specs=(by_rows, by_rows) + (P(),) * 3 + (attn,) * 6 + (P(),) * 9 + (expert,) * 6,
        out_specs=(by_rows, by_rows) + (attn,) * 6 + (P(),) * 9 + (expert,) * 6,
        check_vma=False,
    )
```

```python
import functools
import math

import jax
import jax.numpy as jnp
from jax import lax
from jax.experimental import pallas as pl
from jax.experimental.pallas import tpu as pltpu
from jax.sharding import Mesh
from jax.sharding import PartitionSpec as P

D = 1024
HEADS = 16
FF = 2816
BUCKETS = 32
STEP = 10
QUAD = 4
REP = ("grp", "quad")
PLANE = ("quad", "exp")
ALL = ("grp", "quad", "exp")

highest = lax.Precision.HIGHEST
eps_norm = 1e-06
thresholds = (1, 2, 3, 4, 5, 6, 7, 8, 11, 16, 22, 32, 45, 64, 90)
beta_one = 0.9
beta_two = 0.999
eps_adam = 1e-08
low = jnp.bfloat16
full = jnp.float32
MESH = pl.DeviceIdType.MESH


def adamw_update(weight, moment, second, gradient, step_rate, decay_factor):
    new_moment = beta_one * moment + (1.0 - beta_one) * gradient
    new_second = beta_two * second + (1.0 - beta_two) * gradient * gradient
    corrected = new_moment / (1.0 - beta_one**STEP)
    scaled = new_second / (1.0 - beta_two**STEP)
    new_weight = weight - step_rate * (
        corrected / (jnp.sqrt(scaled) + eps_adam) + decay_factor * weight
    )
    return (new_moment, new_second, new_weight)


def gated_unit(gate_input, up_input):
    return jax.nn.gelu(gate_input, approximate=True) * up_input


def dot(a, b):
    return jnp.dot(a, b, preferred_element_type=full)


def nt(a, b, precision=None):
    return lax.dot_general(a, b, (((1,), (1,)), ((), ())), preferred_element_type=full, precision=precision)


def tn(a, b):
    return lax.dot_general(a, b, (((0,), (0,)), ((), ())), preferred_element_type=full)


class Where:
    def __init__(self, grps, exps):
        self.grps, self.exps = grps, exps
        self.reps = grps * QUAD
        self.grp = lax.axis_index("grp")
        self.quad = lax.axis_index("quad")
        self.exp = lax.axis_index("exp")
        self.rep = self.grp * QUAD + self.quad
        self.base = self.rep * exps
        self.me = self.base + self.exp

    def device(self, rep, exp):
        return (rep // QUAD, rep % QUAD, exp)

    def near(self, flip):
        q = self.quad
        if flip & 1:
            q = q + 1 - 2 * (q % 2)
        if flip & 2:
            q = q + 2 - 4 * (q // 2)
        return q


def send(src, dst, send_sem, recv_sem, device):
    return pltpu.make_async_remote_copy(
        src_ref=src, dst_ref=dst, send_sem=send_sem, recv_sem=recv_sem, device_id=device, device_id_type=MESH
    )


def arrived(ref, sem):
    pltpu.make_async_copy(ref, ref, sem).wait()


def greet(count, device):
    barrier = pltpu.get_barrier_semaphore()

    def one(k, _):
        pl.semaphore_signal(barrier, inc=1, device_id=device(k), device_id_type=MESH)
        return 0

    lax.fori_loop(1, count + 1, one, 0)
    return functools.partial(pl.semaphore_wait, barrier, count)


def everyone(at):
    count = at.reps * at.exps

    def device(k):
        other = (at.me + k) % count
        return at.device(other // at.exps, other % at.exps)

    return count - 1, device


def neighbours(at):
    members = QUAD * at.exps
    plane = at.quad * at.exps + at.exp

    def device(k):
        other = (plane + k) % members
        rest = k - members
        grp = jnp.where(k < members, at.grp, (at.grp + 1 + rest // QUAD) % at.grps)
        quad = jnp.where(k < members, other // at.exps, rest % QUAD)
        return grp, quad, jnp.where(k < members, other % at.exps, at.exp)

    return members - 1 + QUAD * (at.grps - 1), device


def turn(exp, i):
    beside = exp + 1 - 2 * (exp % 2)
    return jnp.where(i == 0, (beside + 2) % 4, jnp.where(i == 1, (exp + 2) % 4, jnp.where(i == 2, beside, exp)))


def lane_of(shape):
    return lax.broadcasted_iota(jnp.int32, shape, 1)


def row_of(shape):
    return lax.broadcasted_iota(jnp.int32, shape, 0)


def bucket_of(offset):
    distance = jnp.abs(offset)
    bucket = jnp.where(offset > 0, 16, 0)
    for threshold in thresholds:
        bucket = bucket + jnp.where(distance >= threshold, 1, 0)
    return bucket


def bits_of(count):
    return count.bit_length() - 1


def column_parts(width):
    tiles = width // 128
    cuts = [0, (tiles + 2) // 3, (2 * tiles + 2) // 3, tiles]
    return [(cuts[i] * 128, (cuts[i + 1] - cuts[i]) * 128) for i in range(3)]


def flipped(place, bit):
    return place + (1 - 2 * ((place // (1 << bit)) % 2)) * (1 << bit)


class Doubling:
    def __init__(self, at, own, every, sems, core_sems, orders):
        self.at, self.own, self.every = at, own, every
        self.sems, self.core_sems, self.orders = sems, core_sems, orders
        self.plane = at.quad * at.exps + at.exp
        self.steps = len(orders[0])
        self.parts = column_parts(own.shape[1])

    def device(self, bit):
        other = flipped(self.plane, bit)
        return (self.at.grp, other // self.at.exps, other % self.at.exps)

    def place(self, part, j):
        p = self.plane
        for i, bit in enumerate(self.orders[part]):
            if (j >> i) & 1:
                p = flipped(p, bit + 1)
        return p

    def block(self, part, p):
        begin, size = self.parts[part]
        return self.every.at[p, :, pl.ds(begin, size)]

    def source(self, part, j):
        begin, size = self.parts[part]
        return self.own.at[:, pl.ds(begin, size)] if j == 0 else self.block(part, self.place(part, j))

    def index(self, step, part, j):
        return part * (1 << self.steps) + (1 << step) - 1 + j

    def copy(self, step, part, j):
        i = self.index(step, part, j)
        return send(
            self.source(part, j),
            self.block(part, self.place(part, j)),
            self.sems.at[0, i],
            self.sems.at[1, i],
            self.device(self.orders[part][step] + 1),
        )

    def core_copy(self, part, j):
        i = part * (1 << self.steps) + j
        return send(
            self.source(part, j),
            self.block(part, self.place(part, j)),
            self.core_sems.at[0, i],
            self.core_sems.at[1, i],
            self.device(0),
        )

    def start(self):
        for part in range(3):
            for step in range(self.steps):
                self.copy(step, part, 0).start()
        for part in range(3):
            self.core_copy(part, 0).start()
        self.keep().start()

    def keep(self):
        return pltpu.make_async_copy(self.own, self.every.at[self.plane], self.core_sems.at[1, 3 << self.steps])

    def next(self, step):
        for part in range(3):
            for j in range(1 << step):
                k = (1 << step) + j
                arrived(self.block(part, self.place(part, k)), self.sems.at[1, self.index(step, part, j)])
                for later in range(step + 1, self.steps):
                    self.copy(later, part, k).start()
                self.core_copy(part, k).start()

    def finish_in(self):
        for part in range(3):
            for j in range(1 << self.steps):
                there = self.block(part, flipped(self.place(part, j), 0))
                arrived(there, self.core_sems.at[1, part * (1 << self.steps) + j])
        self.keep().wait()

    def finish_out(self):
        for part in range(3):
            for j in range(1 << self.steps):
                self.core_copy(part, j).wait_send()
            for step in range(self.steps):
                for j in range(1 << step):
                    self.copy(step, part, j).wait_send()


class Halving:
    def __init__(self, at, bufs, sems, orders):
        self.at, self.bufs, self.sems = at, bufs, sems
        self.plane = at.quad * at.exps + at.exp
        self.places = bits_of(QUAD * at.exps)
        self.chip_bits = list(range(self.places - 1))
        self.parts = column_parts(bufs[0].shape[2])
        self.orders = orders

    def device(self, bit):
        other = flipped(self.plane, bit)
        return (self.at.grp, other // self.at.exps, other % self.at.exps)

    def hop(self, step, part):
        order = self.orders[part]
        bit = order[step]
        left = [b for b in self.chip_bits if b not in order[:step]]
        pos = left.index(bit)
        half = 1 << (len(left) - 1)
        mine = (self.plane // (1 << (bit + 1))) % 2
        device = self.device(bit + 1)
        begin, size = self.parts[part]
        cols = pl.ds(begin, size)
        base = self.base(step, part)

        def index(j, value):
            return (j >> pos) * (1 << (pos + 1)) + value * (1 << pos) + j % (1 << pos)

        pairs = []
        for j in range(half):
            copy = functools.partial(
                send,
                self.bufs[step].at[index(j, 1 - mine), :, cols],
                self.bufs[step + 1].at[j, :, cols],
                self.sems.at[0, base + j],
                self.sems.at[1, base + j],
                device,
            )
            pairs.append((copy, index(j, mine), j))
        return pairs, begin, size, base

    def base(self, step, part):
        n = len(self.chip_bits)
        return part * (1 << n) + sum(1 << (n - 1 - s) for s in range(step))

    def start(self, step, part=None):
        for p in range(3) if part is None else [part]:
            for copy, _, _ in self.hop(step, p)[0]:
                copy().start()

    def add(self, step, part):
        pairs, begin, size, base = self.hop(step, part)
        cols = pl.ds(begin, size)
        here, there = self.bufs[step], self.bufs[step + 1]
        for _, keep, j in pairs:
            arrived(there.at[j, :, cols], self.sems.at[1, base + j])
            there[j, :, begin : begin + size] = (
                there[j, :, begin : begin + size] + here[keep, :, begin : begin + size]
            )

    def next(self, step):
        for p in range(3):
            self.add(step, p)
            if step + 1 < len(self.chip_bits):
                self.start(step + 1, p)

    def result(self):
        return self.bufs[len(self.chip_bits)]

    def finish(self):
        for step in range(len(self.chip_bits)):
            for p in range(3):
                for copy, _, _ in self.hop(step, p)[0]:
                    copy().wait_send()


class Group:
    def __init__(self, at, own, every, sems):
        self.at, self.own, self.every, self.sems = at, own, every, sems
        self.beside, self.across = at.exp + 1 - 2 * (at.exp % 2), (at.exp + 2) % 4

    def copy(self, src, index, send_index, device):
        return send(
            src, self.every.at[index], self.sems.at[0, send_index], self.sems.at[1, index], self.at.device(self.at.rep, device)
        )

    def first(self):
        return [
            self.copy(self.own, self.at.exp, 0, self.across),
            self.copy(self.own, self.at.exp, 1, self.beside),
        ]

    def second(self):
        return self.copy(self.every.at[self.across], self.across, 2, self.beside)

    def start(self):
        for copy in self.first():
            copy.start()

    def pass_on(self):
        arrived(self.every.at[self.across], self.sems.at[1, self.across])
        self.second().start()

    def arrive(self):
        for index in (self.beside, (self.beside + 2) % 4):
            arrived(self.every.at[index], self.sems.at[1, index])

    def sent(self):
        for copy in self.first() + [self.second()]:
            copy.wait_send()


class Tiles:
    def __init__(self, units, reps):
        self.units = units
        self.reps = reps
        self.hidden = units * reps
        self.half = self.hidden // 256
        self.wide = (self.half + 1) // 2
        self.count = 3
        self.size = 128 * self.wide // self.count
        self.skip = 128 * (2 * self.wide - self.half)

    def start(self, quad):
        return 128 * (self.half * (quad // 2) + (self.half - self.wide) * (quad % 2))

    def rows(self, tile):
        result = []
        for k in range(QUAD):
            found = None
            for parity in range(2):
                first = self.start(parity) + tile * self.size
                live = first + (self.skip if parity and tile == 0 else 0)
                begin = max(live, k * self.units)
                end = min(first + self.size, (k + 1) * self.units)
                if end > begin:
                    found = (begin - k * self.units, end - begin, parity, begin - first)
            result.append(found)
        return result


class Outward:
    def __init__(self, at, tiles, tile, in_low, down_slab, both_w, down_w, nothing, sems, down_sems):
        self.at, self.tiles, self.tile = at, tiles, tile
        self.in_low, self.down_slab, self.both_w, self.down_w = in_low, down_slab, both_w, down_w
        self.nothing, self.sems, self.down_sems = nothing, sems, down_sems
        self.slab = in_low.shape[0]

    def source(self, quad, section):
        begin = section * self.tiles.hidden + self.tiles.start(quad) + self.tile * self.tiles.size
        return self.in_low.at[:, pl.ds(pl.multiple_of(begin, 128), self.tiles.size)]

    def target(self, rep, section):
        rows = pl.ds(pl.multiple_of(rep * self.slab, self.slab), self.slab)
        return self.both_w.at[rows, pl.ds(section * self.tiles.size, self.tiles.size)]

    def over(self, act):
        at = self.at

        def one(k, _):
            other = (at.rep + k) % at.reps
            for section in range(2):
                act(
                    functools.partial(
                        send,
                        self.source(other % QUAD, section),
                        self.target(at.rep, section),
                        self.sems.at[0, section * at.reps + other],
                        self.sems.at[1, section * at.reps + at.rep],
                        at.device(other, at.exp),
                    )
                )
            return 0

        lax.fori_loop(1, at.reps, one, 0)

    def over_down(self, act, act_local):
        at = self.at
        for k, piece in enumerate(self.tiles.rows(self.tile)):
            if piece is None:
                continue
            begin, count, parity, to = piece
            quad = 2 * (at.rep // QUAD) + parity
            src, dst = self.down_slab.at[pl.ds(begin, count)], self.down_w.at[pl.ds(to, count)]
            recv = self.down_sems.at[1, at.rep]
            for g in range(at.grps):
                stays = jnp.logical_and(at.grp == g, at.quad == quad)
                ours = at.rep % QUAD == k

                @pl.when(jnp.logical_and(ours, jnp.logical_not(stays)))
                def _():
                    act(functools.partial(send, src, dst, self.down_sems.at[0, g], recv, (g, quad, at.exp)))

                @pl.when(jnp.logical_and(ours, stays))
                def _():
                    act_local(functools.partial(pltpu.make_async_copy, src, dst, recv))

    def blank(self):
        return pltpu.make_async_copy(
            self.nothing, self.down_w.at[pl.ds(0, self.tiles.skip)], self.down_sems.at[1, self.at.reps]
        )

    def start(self):
        at = self.at
        self.over_down(lambda copy: copy().start(), lambda copy: copy().start())
        self.over(lambda copy: copy().start())
        for section in range(2):
            pltpu.make_async_copy(
                self.source(at.quad, section), self.target(at.rep, section), self.sems.at[1, section * at.reps + at.rep]
            ).start()
        if self.tile == 0:

            @pl.when(at.quad % 2 == 1)
            def _():
                self.blank().start()

    def arrive(self):
        at = self.at

        def one(rep, _):
            for section in range(2):
                arrived(self.target(rep, section), self.sems.at[1, section * at.reps + rep])
            return 0

        lax.fori_loop(0, at.reps, one, 0)
        for parity in range(2):

            @pl.when(at.quad % 2 == parity)
            def _():
                for k, piece in enumerate(self.tiles.rows(self.tile)):
                    if piece is not None and piece[2] == parity:
                        source = QUAD * (at.quad // 2) + k
                        arrived(self.down_w.at[pl.ds(piece[3], piece[1])], self.down_sems.at[1, source])
                if parity and self.tile == 0:
                    self.blank().wait()

    def sent(self):
        self.over(lambda copy: copy().wait_send())
        self.over_down(lambda copy: copy().wait_send(), lambda copy: None)


class Homeward:
    def __init__(self, at, tiles, tile, both, down, in_parts, down_parts, sems, down_sems, sections=(0, 1)):
        self.at, self.tiles, self.tile, self.sections = at, tiles, tile, sections
        self.both, self.down, self.in_parts, self.down_parts = both, down, in_parts, down_parts
        self.sems, self.down_sems = sems, down_sems
        self.slab = in_parts.shape[1]

    def target(self, grp, quad, parity, section):
        skip = self.tiles.skip if parity and self.tile == 0 else 0
        to = section * self.tiles.hidden + self.tiles.start(quad) + self.tile * self.tiles.size + skip
        to = to if isinstance(to, int) else pl.multiple_of(to, 128)
        return skip, self.in_parts.at[grp, :, pl.ds(to, self.tiles.size - skip)]

    def copy(self, rep, parity, section, local=False):
        at = self.at
        skip, dst = self.target(at.grp, at.quad, parity, section)
        rows = pl.ds(pl.multiple_of(rep * self.slab, self.slab), self.slab)
        src = self.both.at[rows, pl.ds(section * self.tiles.size + skip, self.tiles.size - skip)]
        recv = self.sems.at[1, section * at.reps + at.rep]
        if local:
            return pltpu.make_async_copy(src, dst, recv)
        return send(src, dst, self.sems.at[0, section * at.reps + rep], recv, at.device(rep, at.exp))

    def over(self, act, act_local):
        at = self.at
        for parity in range(2):

            @pl.when(at.quad % 2 == parity)
            def _():
                def one(k, _):
                    for section in self.sections:
                        act(self.copy((at.rep + k) % at.reps, parity, section))
                    return 0

                lax.fori_loop(1, at.reps, one, 0)
                if act_local:
                    for section in self.sections:
                        act_local(self.copy(at.rep, parity, section, local=True))

    def over_down(self, act, act_local):
        at = self.at
        if self.down is None:
            return
        for k, piece in enumerate(self.tiles.rows(self.tile)):
            if piece is None:
                continue
            begin, count, parity, to = piece
            src, dst = self.down.at[pl.ds(to, count)], self.down_parts.at[at.grp, pl.ds(begin, count)]
            recv = self.down_sems.at[1, at.grp]
            stays = jnp.logical_and(at.grp == at.quad // 2, at.quad == k)
            ours = at.quad % 2 == parity

            @pl.when(jnp.logical_and(ours, jnp.logical_not(stays)))
            def _():
                act(functools.partial(send, src, dst, self.down_sems.at[0, k], recv, (at.quad // 2, k, at.exp)))

            @pl.when(jnp.logical_and(ours, stays))
            def _():
                act_local(functools.partial(pltpu.make_async_copy, src, dst, recv))

    def start(self):
        self.over_down(lambda copy: copy().start(), lambda copy: copy().start())
        self.over(lambda copy: copy.start(), lambda copy: copy.start())

    def arrive(self):
        at = self.at
        for rep in range(at.reps):
            for section in self.sections:
                _, dst = self.target(rep // QUAD, rep % QUAD, rep % 2, section)
                arrived(dst, self.sems.at[1, section * at.reps + rep])
        for k, piece in enumerate(self.tiles.rows(self.tile)):
            if piece is None or self.down is None:
                continue

            @pl.when(at.quad == k)
            def _():
                for g in range(at.grps):
                    arrived(self.down_parts.at[g, pl.ds(piece[0], piece[1])], self.down_sems.at[1, g])

    def sent(self):
        self.over(lambda copy: copy.wait_send(), None)
        self.over_down(lambda copy: copy().wait_send(), lambda copy: None)


def forward_kernel(
    grps,
    exps,
    lengths,
    bias_table,
    routes_t,
    tokens,
    cotangent,
    gains,
    router,
    attn_qkv,
    attn_out,
    expert_in,
    expert_out,
    both_w,
    down_w,
    cot_all,
    n_all,
    comb_all,
    qkv_out,
    pb_out,
    mine_out,
    n1_out,
    wqkv_out,
    wout_out,
    h1_out,
    n2_out,
    probs_out,
    in_out,
    down_out,
    in_wide,
    down_wide,
    qkv_t,
    out_w,
    in_low,
    down_slab,
    tok_all,
    wqkv,
    wout,
    n1,
    qkv,
    pb,
    mine,
    ctx,
    bias,
    comb_send,
    nothing,
    tok_sem,
    wq_sem,
    wo_sem,
    wo2_sem,
    weight_sem,
    down_sem,
    ctx_sem,
    cot_sem,
    cot_core_sem,
    n_sem,
    n_core_sem,
    comb_sem,
    store_sem,
    cast_sem,
):
    at = Where(grps, exps)
    reps = at.reps
    rows, width = tokens.shape
    heads = HEADS // exps
    head_dim = width // HEADS
    head_cols = heads * head_dim
    block_cols = min(128, head_cols)
    shard_cols, row_block = qkv_t.shape
    seg = math.gcd(shard_cols, head_cols)
    segs = shard_cols // seg
    tiles = Tiles(down_slab.shape[0], reps)
    plane = at.quad * exps + at.exp
    members = QUAD * exps
    scale = 1.0 / math.sqrt(head_dim)
    SEND, RECV = 0, 1

    met = greet(*everyone(at))
    wide_copies = [
        pltpu.make_async_copy(expert_in, in_wide, cast_sem.at[0]),
        pltpu.make_async_copy(expert_out, down_wide, cast_sem.at[1]),
    ]
    for copy in wide_copies:
        copy.start()
    qkv_t[...] = attn_qkv[...].T.astype(low)
    out_w[...] = attn_out[...].astype(low)
    met()

    def exp_peer(k):
        return (at.exp + k) % exps

    group_tokens = Group(at, tokens, tok_all, tok_sem)
    group_tokens.start()
    tok_all[at.exp] = tokens[...]

    def segment(k):
        col = (at.rep * segs + k) * seg
        section = col // width
        within = col - section * width
        owner = within // head_cols
        return owner, section * head_cols + within - owner * head_cols

    def segment_copy(k, shift):
        owner, offset = segment(k)
        src = qkv_t.at[pl.ds(k * seg, seg)]
        dst = wqkv.at[at.exp, pl.ds(pl.multiple_of(offset, seg), seg)]
        target = at.device((at.rep + shift) % reps, owner)
        return owner, src, dst, functools.partial(
            send, src, dst, wq_sem.at[SEND, k * reps + shift], wq_sem.at[RECV, at.exp * 3 * (head_cols // seg) + offset // seg], target
        )

    def over_segments(act, act_local):
        def one(i, _):
            k, shift = i // reps, i % reps
            owner, src, dst, copy = segment_copy(k, shift)
            stays = jnp.logical_and(shift == 0, owner == at.exp)

            @pl.when(jnp.logical_not(stays))
            def _():
                act(copy())

            @pl.when(stays)
            def _():
                act_local(k, src, dst)

            return 0

        lax.fori_loop(0, segs * reps, one, 0)

    def local_segment(k, src, dst):
        _, offset = segment(k)
        pltpu.make_async_copy(src, dst, wq_sem.at[RECV, at.exp * 3 * (head_cols // seg) + offset // seg]).start()

    over_segments(lambda copy: copy.start(), local_segment)

    for k in range(1, reps):
        other = (at.rep + k) % reps
        send(
            out_w, wout.at[at.exp, at.rep], wo_sem.at[SEND, other], wo_sem.at[RECV, at.rep], at.device(other, at.exp)
        ).start()
    wout[at.exp, at.rep] = out_w[...]
    chip_bits = list(range(bits_of(members) - 1))
    cots = Doubling(at, cotangent, cot_all, cot_sem, cot_core_sem, [chip_bits[::-1]] * 3)
    cots.start()

    span = 2 * rows
    bucket = bucket_of(lane_of((8, span)) - rows)
    for h in range(heads):
        line = jnp.zeros((8, span), full)
        for b in range(BUCKETS):
            line = jnp.where(bucket == b, bias_table[at.exp * heads + h, b], line)
        whole = jnp.broadcast_to(line[0:1], (rows, span))
        bias[h] = pltpu.roll(whole, 0, 1, stride=1, stride_axis=0)[:, rows:]

    group_tokens.pass_on()
    group_tokens.arrive()

    def norm_group(s, _):
        x = tok_all[s].astype(full)
        r = lax.rsqrt(jnp.mean(x * x, axis=1, keepdims=True) + eps_norm)
        n1[s] = (x * r * gains[0:1, :]).astype(low)
        return 0

    lax.fori_loop(0, exps, norm_group, 0)

    for copy in wide_copies:
        copy.wait()
    in_low[...] = in_wide[...].astype(low)
    down_slab[...] = down_wide[...].astype(low)
    nothing[...] = jnp.zeros_like(nothing)
    weights = [
        Outward(
            at, tiles, t, in_low, down_slab, both_w.at[t], down_w.at[t], nothing, weight_sem.at[t], down_sem.at[t]
        )
        for t in range(2)
    ]

    weights[0].start()

    def wait_segment(i, _):
        e, j = i // (3 * head_cols // seg), i % (3 * head_cols // seg)
        arrived(wqkv.at[e, pl.ds(pl.multiple_of(j * seg, seg), seg)], wq_sem.at[RECV, i])
        return 0

    lax.fori_loop(0, exps * 3 * head_cols // seg, wait_segment, 0)

    def project(s, _):
        total = jnp.zeros((rows, 3 * head_cols), full)
        for e in range(exps):
            total = total + nt(n1[s, :, e * row_block : (e + 1) * row_block], wqkv[e])
        qkv[s] = total.astype(low)
        return 0

    lax.fori_loop(0, exps, project, 0)

    group_wout = Group(at, wout.at[at.exp], wout, wo2_sem)

    def beside(k):
        if k == 1:
            for j in range(1, reps):
                other = (at.rep + j) % reps
                arrived(wout.at[at.exp, other], wo_sem.at[RECV, other])
            group_wout.start()
        elif k == 2:
            cots.next(0)
        else:
            group_wout.pass_on()

    def attend(i, _):
        s = turn(at.exp, i)
        for k in range(1, exps):

            @pl.when(i == k)
            def _():
                beside(k)

        ok = lane_of((rows, rows)) < lengths[at.base + s]
        lane = lane_of((rows, block_cols))
        for c in range(head_cols // block_cols):
            cols = slice(c * block_cols, (c + 1) * block_cols)
            q = qkv[s, :, cols] * scale
            k = qkv[s, :, head_cols + c * block_cols : head_cols + (c + 1) * block_cols]
            v = qkv[s, :, 2 * head_cols + c * block_cols : 2 * head_cols + (c + 1) * block_cols]
            result = jnp.zeros((rows, block_cols), full)
            for t in range(block_cols // head_dim):
                h = c * (block_cols // head_dim) + t
                here = jnp.logical_and(lane >= t * head_dim, lane < (t + 1) * head_dim)
                scores = nt(jnp.where(here, q, jnp.zeros_like(q)), k) + bias[h]
                scores = jnp.where(ok, scores, -1e30)
                top = jnp.max(scores, axis=1, keepdims=True)
                weights = jnp.exp(scores - top)
                total = jnp.sum(weights, axis=1, keepdims=True)
                weights = (weights * (1.0 / total)).astype(low)
                result = jnp.where(here, jnp.dot(weights, v, preferred_element_type=full), result)
                pb[s * heads + h] = weights
            mine[s, :, cols] = result.astype(low)

        @pl.when(i < exps - 1)
        def _():
            send(
                mine.at[s], ctx.at[at.exp], ctx_sem.at[SEND, s], ctx_sem.at[RECV, at.exp], at.device(at.rep, s)
            ).start()

        @pl.when(i == exps - 1)
        def _():
            pltpu.make_async_copy(mine.at[s], ctx.at[at.exp], ctx_sem.at[RECV, at.exp]).start()

        return 0

    lax.fori_loop(0, exps, attend, 0)

    cots.next(1)
    group_wout.arrive()
    for e in range(exps):
        arrived(ctx.at[e], ctx_sem.at[RECV, e])

    out_cols = wout.shape[3]
    for r in range(reps):
        cols = slice(r * out_cols, (r + 1) * out_cols)
        total = tokens[:, cols].astype(full)
        for e in range(exps):
            total = total + jnp.dot(ctx[e], wout[e, r], preferred_element_type=full)
        h1_out[:, cols] = total
    h1 = h1_out[...]
    r2 = lax.rsqrt(jnp.mean(h1 * h1, axis=1, keepdims=True) + eps_norm)
    n2 = (h1 * r2 * gains[1:2, :]).astype(low)
    n2_out[...] = n2
    rotated = [chip_bits[c:] + chip_bits[:c] for c in range(3)]
    rows_two = Doubling(at, n2_out, n_all, n_sem, n_core_sem, rotated)
    rows_two.start()
    weights[1].start()

    router_rows = jnp.concatenate([router[...], jnp.zeros((128 - exps, width), full)], axis=0)
    logits = nt(n2.astype(full), router_rows, precision=highest)
    lane = lane_of((rows, 128))
    logits = jnp.where(lane < exps, logits, -1e30)
    probs = jnp.exp(logits - jnp.max(logits, axis=1, keepdims=True))
    probs = probs / jnp.sum(probs, axis=1, keepdims=True)
    probs_out[...] = probs
    picked = jnp.where(routed(routes_t, at.me, rows), probs, 0.0)
    comb = picked / jnp.sum(picked, axis=1, keepdims=True)
    comb = jnp.where(row_of((rows, 1)) < lengths[at.me], comb, 0.0)
    comb_send[...] = comb.T[0 : comb_send.shape[0]]

    def comb_copy(k):
        other = (plane + k) % members
        return send(
            comb_send,
            comb_all.at[plane],
            comb_sem.at[SEND, other],
            comb_sem.at[RECV, plane],
            (at.grp, other // exps, other % exps),
        )

    def start_comb(k, _):
        comb_copy(k).start()
        return 0

    lax.fori_loop(1, members, start_comb, 0)
    pltpu.make_async_copy(comb_send, comb_all.at[plane], comb_sem.at[RECV, plane]).start()
    rows_two.next(0)

    stores = [
        (qkv, qkv_out),
        (pb, pb_out),
        (mine, mine_out),
        (n1, n1_out),
        (wqkv, wqkv_out),
        (wout, wout_out),
        (in_low, in_out),
        (down_slab, down_out),
    ]
    for i, (src, dst) in enumerate(stores):
        pltpu.make_async_copy(src, dst, store_sem.at[i]).start()

    for step in range(1, rows_two.steps):
        rows_two.next(step)
    for step in range(2, cots.steps):
        cots.next(step)

    cots.finish_in()
    rows_two.finish_in()

    def comb_in(k, _):
        arrived(comb_all.at[k], comb_sem.at[RECV, k])
        return 0

    lax.fori_loop(0, members, comb_in, 0)
    for tile in weights:
        tile.arrive()

    for k in range(1, exps):
        peer = exp_peer(k)
        arrived(mine.at[peer], ctx_sem.at[SEND, peer])
    over_segments(lambda copy: copy.wait_send(), lambda k, src, dst: None)
    for k in range(1, reps):
        arrived(out_w, wo_sem.at[SEND, (at.rep + k) % reps])
    group_tokens.sent()
    group_wout.sent()
    cots.finish_out()
    rows_two.finish_out()

    def sent_comb(k, _):
        comb_copy(k).wait_send()
        return 0

    lax.fori_loop(1, members, sent_comb, 0)
    for tile in weights:
        tile.sent()
    for i, (src, dst) in enumerate(stores):
        pltpu.make_async_copy(src, dst, store_sem.at[i]).wait()


def forward_call(
    grps, exps, lengths, bias_table, routes_t, tokens, cotangent, gains, router, attn_qkv, attn_out, expert_in, expert_out
):
    reps = grps * QUAD
    rows, width = tokens.shape
    head_cols = width // exps
    row_block, shard_cols = attn_qkv.shape
    seg = math.gcd(shard_cols, head_cols)
    segs = shard_cols // seg
    units = expert_out.shape[0]
    out_cols = attn_out.shape[1]
    heads = HEADS // exps
    members = QUAD * exps
    tiles = Tiles(units, reps)
    shape = jax.ShapeDtypeStruct
    vmem = pl.BlockSpec(memory_space=pltpu.VMEM)
    smem = pl.BlockSpec(memory_space=pltpu.SMEM)
    hbm = pl.BlockSpec(memory_space=pl.ANY)
    results = [
        (shape((2, width, 2 * tiles.size), low), hbm),
        (shape((2, tiles.size, width), low), hbm),
        (shape((members, rows, width), low), hbm),
        (shape((members, rows, width), low), hbm),
        (shape((members, 8, rows), full), hbm),
        (shape((exps, rows, 3 * head_cols), low), hbm),
        (shape((exps * heads, rows, rows), low), hbm),
        (shape((exps, rows, head_cols), low), hbm),
        (shape((exps, rows, width), low), hbm),
        (shape((exps, 3 * head_cols, row_block), low), hbm),
        (shape((exps, reps, row_block, out_cols), low), hbm),
        (shape((rows, width), full), vmem),
        (shape((rows, width), low), vmem),
        (shape((rows, 128), full), vmem),
        (shape(expert_in.shape, low), hbm),
        (shape(expert_out.shape, low), hbm),
    ]
    dma = pltpu.SemaphoreType.DMA
    chips = members // 2
    return pl.pallas_call(
        functools.partial(forward_kernel, grps, exps),
        out_shape=[r[0] for r in results],
        in_specs=[smem] * 2 + [vmem] * 7 + [hbm] * 2,
        out_specs=[r[1] for r in results],
        scratch_shapes=[
            pltpu.VMEM(expert_in.shape, full),
            pltpu.VMEM(expert_out.shape, full),
            pltpu.VMEM((shard_cols, row_block), low),
            pltpu.VMEM((row_block, out_cols), low),
            pltpu.VMEM(expert_in.shape, low),
            pltpu.VMEM(expert_out.shape, low),
            pltpu.VMEM((exps, rows, width), low),
            pltpu.VMEM((exps, 3 * head_cols, row_block), low),
            pltpu.VMEM((exps, reps, row_block, out_cols), low),
            pltpu.VMEM((exps, rows, width), low),
            pltpu.VMEM((exps, rows, 3 * head_cols), low),
            pltpu.VMEM((exps * heads, rows, rows), low),
            pltpu.VMEM((exps, rows, head_cols), low),
            pltpu.VMEM((exps, rows, head_cols), low),
            pltpu.VMEM((heads, rows, rows), full),
            pltpu.VMEM((8, rows), full),
            pltpu.VMEM((tiles.skip, width), low),
            dma((2, exps)),
            dma((2, max(segs * reps, exps * 3 * head_cols // seg))),
            dma((2, reps)),
            dma((2, exps)),
            dma((2, 2, 2 * reps)),
            dma((2, 2, reps + 1)),
            dma((2, exps)),
            dma((2, 3 * chips)),
            dma((2, 3 * chips + 1)),
            dma((2, 3 * chips)),
            dma((2, 3 * chips + 1)),
            dma((2, members)),
            dma((8,)),
            dma((2,)),
        ],
        compiler_params=pltpu.CompilerParams(
            collective_id=0, has_side_effects=True, vmem_limit_bytes=60 * 1024 * 1024
        ),
        name="forward",
    )(lengths, bias_table, routes_t, tokens, cotangent, gains, router, attn_qkv, attn_out, expert_in, expert_out)


def expert_kernel(
    grps,
    exps,
    cap,
    deal,
    routes_t,
    comb,
    n_all,
    cot_all,
    both_w,
    down_w,
    in_low,
    down_slab,
    h1,
    n_total,
    y_half,
    y_far,
    c_in,
    both_g,
    down_g,
    in_parts,
    down_parts,
    place,
    marks,
    n_rows,
    g_rows,
    both_v,
    down_v,
    raw_n,
    raw_g,
    y_acc,
    n_acc,
    both_d,
    active,
    n_bufs,
    c_sum,
    out_y,
    load_sem,
    raw_sem,
    out_sem,
    in_sem,
    in_down_sem,
    home_sem,
    home_down_sem,
    stage_sem,
    far_sem,
    n_sem,
    c_sem,
):
    at = Where(grps, exps)
    rows, width = n_all.shape[1:]
    tiles = Tiles(down_slab.shape[0], at.reps)
    size = tiles.size
    slots = exps * cap
    members = QUAD * exps
    loads = [pltpu.make_async_copy(both_w.at[t], both_v.at[t], load_sem.at[0, t]) for t in range(2)] + [
        pltpu.make_async_copy(down_w.at[t], down_v.at[t], load_sem.at[1, t]) for t in range(2)
    ]
    for copy in loads:
        copy.start()

    def raw_copies(q):
        here = pl.ds(pl.multiple_of(q * exps, exps), exps)
        return [
            pltpu.make_async_copy(n_all.at[here], raw_n.at[pl.ds(q % 2 * exps, exps)], raw_sem.at[0, q % 2]),
            pltpu.make_async_copy(cot_all.at[here], raw_g.at[pl.ds(q % 2 * exps, exps)], raw_sem.at[1, q % 2]),
        ]

    for copy in raw_copies(0):
        copy.start()

    beside = at.exp + 1 - 2 * (at.exp % 2)
    greet(*neighbours(at))()
    last = tiles.count - 1
    incoming = Outward(
        at, tiles, last, in_low, down_slab, both_v.at[last], down_v.at[last], None, in_sem, in_down_sem
    )
    incoming.start()
    home = Homeward(
        at, tiles, 0, both_v.at[0], down_v.at[0], in_parts, down_parts, home_sem, home_down_sem, (0,)
    )

    earlier = jnp.where(row_of((rows, rows)) < lane_of((rows, rows)), 1.0, 0.0).astype(low)
    slot = row_of((cap, rows)).astype(full)

    def dispatch(q, _):
        @pl.when(q + 1 < QUAD)
        def _():
            for copy in raw_copies(q + 1):
                copy.start()

        for copy in raw_copies(q):
            copy.wait()
        lines = []
        for j in range(exps):
            seq = at.grp * members + q * exps + j
            pair = routes_t[:, pl.ds(pl.multiple_of(seq * rows, rows), rows)]
            lines.append(jnp.logical_or(pair[0:1] == at.exp, pair[1:2] == at.exp))
        lines = [jnp.where(line, 1.0, 0.0) for line in lines] + [jnp.zeros((8 - exps, rows), full)]
        hot_low = jnp.concatenate(lines, axis=0).astype(low)
        before = dot(hot_low, earlier)
        for j in range(exps):
            s = q * exps + j
            inside = jnp.logical_and(slot == before[j : j + 1, :], hot_low[j : j + 1, :].astype(full) > 0.5)
            here = jnp.where(inside, 1.0, 0.0)
            place[s] = here.astype(low)
            g = raw_g[q % 2 * exps]
            for b in range(1, exps):
                g = jnp.where(deal[at.grp * members + s] == at.grp * members + q * exps + b, raw_g[q % 2 * exps + b], g)
            where = pl.ds(pl.multiple_of(s * cap, cap), cap)
            n_rows[where] = dot(here.astype(low), raw_n[q % 2 * exps + j]).astype(low)
            g_rows[where] = dot(here.astype(low), g).astype(low)
            marks[where, 0:1] = jnp.sum(here * comb[s, pl.ds(at.exp, 1), :], axis=1, keepdims=True)
            marks[where, 1:2] = jnp.zeros((cap, 1), full)
        return 0

    lax.fori_loop(0, QUAD, dispatch, 0)
    for copy in loads:
        copy.wait()
    curve = math.sqrt(2.0 / math.pi)

    core = at.exp % 2

    plane = at.quad * exps + at.exp
    sibling = at.device(at.rep, beside)
    dn = Halving(at, n_bufs, n_sem, [[0, 1, 2], [1, 2, 0], [2, 0, 1]])

    def n_copy(j):
        return send(raw_n.at[j], n_bufs[0].at[j], far_sem.at[0, 0, j], far_sem.at[0, 1, j], sibling)

    def y_copies(j):
        return (
            pltpu.make_async_copy(out_y.at[j % 2], y_half.at[j], out_sem.at[j % 2]),
            send(raw_n.at[j], y_far.at[j], far_sem.at[1, 0, j], far_sem.at[1, 1, j], sibling),
        )

    def c_copy(k):
        other = (plane + k) % members
        return send(
            c_sum.at[other],
            c_in.at[plane],
            c_sem.at[0, other],
            c_sem.at[1, plane],
            (at.grp, other // exps, other % exps),
        )

    def slots_of(s):
        return pl.ds(pl.multiple_of(s * cap, cap), cap)

    def n_rows_of(s):
        where = slots_of(s)
        line = jnp.sum(place[s].astype(full) * marks[where, 1:2], axis=0, keepdims=True)
        c_sum[s] = jnp.broadcast_to(line, (8, rows))
        return tn(place[s], n_acc[where]).astype(low)

    def y_rows_of(p):
        first = p // exps * exps
        spot = at.grp * members + p
        here, y = place[first], y_acc[slots_of(first)]
        for c in range(1, exps):
            taken = deal[at.grp * members + first + c] == spot
            here = jnp.where(taken, place[first + c], here)
            y = jnp.where(taken, y_acc[slots_of(first + c)], y)
        return (tn(here, y) + jnp.where(deal[at.me] == spot, h1[...], 0.0)).astype(low)

    def give_n(j):
        raw_n[j] = n_rows_of(2 * j + 1 - core)
        n_copy(j).start()
        raw_g[j] = n_rows_of(2 * j + core)

    def add_n(quad):
        for k in range(exps // 2):
            j = quad * (exps // 2) + k
            arrived(n_bufs[0].at[j], far_sem.at[0, 1, j])
            n_bufs[0][j] = n_bufs[0][j] + raw_g[j]

    def give_y(j, _):
        @pl.when(j >= 2)
        def _():
            y_copies(j - 2)[0].wait()

        out_y[j % 2] = y_rows_of(2 * j + core)
        n_copy(j).wait_send()
        raw_n[j] = y_rows_of(2 * j + 1 - core)
        for copy in y_copies(j):
            copy.start()
        return 0

    def start_c(k, _):
        c_copy(k).start()
        return 0

    def tile_work(f, _):
        @pl.when(f == last)
        def _():
            incoming.arrive()
            home.start()

        def chunk(i, _):
            c = jnp.where(i == 0, at.near(3), jnp.where(i == 1, at.near(1), jnp.where(i == 2, at.near(2), at.quad)))
            here = pl.ds(pl.multiple_of(c * slots, slots), slots)
            share = marks[here, 0:1]
            both = dot(n_rows[here], both_v[f])
            gate_part, up_part = both[:, :size], both[:, size:]
            grad = nt(g_rows[here], down_v[f])
            square = gate_part * gate_part
            bend = jnp.tanh(curve * gate_part * (1.0 + 0.044715 * square))
            half = 0.5 * (1.0 + bend)
            gelu = gate_part * half
            slope = half + (0.5 * curve) * gate_part * (1.0 - bend * bend) * (1.0 + (3 * 0.044715) * square)
            value = gelu * up_part
            marks[here, 1:2] += jnp.sum(value * grad, axis=1, keepdims=True)
            grad = grad * share
            active[f % 2, here] = (value * share).astype(low)
            both_d[f % 2, here, :size] = (grad * up_part * slope).astype(low)
            both_d[f % 2, here, size:] = (grad * gelu).astype(low)
            y = dot(active[f % 2, here], down_v[f])
            y_acc[here] = jnp.where(f == 0, y, y_acc[here].astype(full) + y).astype(low)
            n_back = nt(both_d[f % 2, here], both_v[f])
            n_acc[here] = jnp.where(f == 0, n_back, n_acc[here].astype(full) + n_back).astype(low)

            @pl.when(f == last)
            def _():
                for k in range(exps // 2):
                    give_n(c * (exps // 2) + k)

            @pl.when(jnp.logical_and(f == last, i == 2))
            def _():
                add_n(at.near(3))

            @pl.when(jnp.logical_and(f == last, i == 3))
            def _():
                add_n(at.near(1))
                dn.start(0, 1)

            return 0

        lax.fori_loop(0, QUAD, chunk, 0)

        @pl.when(f == 0)
        def _():
            weight_work(0)

        return 0

    def weight_work(f):
        def columns(m, _):
            cols = pl.ds(pl.multiple_of(m * (width // 2), width // 2), width // 2)
            both_v[f, cols] = tn(n_rows[:, cols], both_d[f % 2]).astype(low)
            down_v[f, :, cols] = tn(active[f % 2], g_rows[:, cols]).astype(low)
            return 0

        lax.fori_loop(0, 2, columns, 0)

        for copy in stage_copies(f):
            copy.start()

    def stage_copies(f):
        copies = [pltpu.make_async_copy(both_v.at[f], both_g.at[f], stage_sem.at[0, f])]
        if f:
            copies.append(pltpu.make_async_copy(down_v.at[f], down_g.at[f - 1], stage_sem.at[1, f]))
        return copies

    lax.fori_loop(0, tiles.count, tile_work, 0)

    half = members // 2
    lax.fori_loop(1, members, start_c, 0)
    c_in[plane] = c_sum[plane]
    weight_work(1)
    add_n(at.near(2))
    dn.start(0, 2)
    add_n(at.quad)
    dn.start(0, 0)
    weight_work(2)
    lax.fori_loop(0, half, give_y, 0)
    for step in range(len(dn.chip_bits)):
        dn.next(step)
    n_total[...] = dn.result()[0]
    for j in (half - 2, half - 1):
        y_copies(j)[0].wait()
    for f in range(tiles.count):
        for copy in stage_copies(f):
            copy.wait()

    def core_in(j, _):
        y_copies(j)[1].wait_send()
        arrived(y_far.at[j], far_sem.at[1, 1, j])
        return 0

    lax.fori_loop(0, half, core_in, 0)

    def c_done(k, _):
        c_copy(k).wait_send()
        other = (plane + k) % members
        arrived(c_in.at[other], c_sem.at[1, other])
        return 0

    lax.fori_loop(1, members, c_done, 0)
    dn.finish()
    home.arrive()
    incoming.sent()
    home.sent()


def expert_call(grps, exps, cap, deal, routes_t, comb_all, n_all, cot_all, both_w, down_w, in_low, down_slab, h1):
    members, rows, width = n_all.shape
    reps = grps * QUAD
    tiles = Tiles(down_slab.shape[0], reps)
    size = tiles.size
    slab, both_hidden = in_low.shape
    units = down_slab.shape[0]
    slots = exps * cap
    chip_bits = bits_of(members) - 1
    shape = jax.ShapeDtypeStruct
    vmem = pl.BlockSpec(memory_space=pltpu.VMEM)
    smem = pl.BlockSpec(memory_space=pltpu.SMEM)
    hbm = pl.BlockSpec(memory_space=pl.ANY)
    results = [
        (shape((rows, width), low), vmem),
        (shape((members // 2, rows, width), low), hbm),
        (shape((members // 2, rows, width), low), hbm),
        (shape((members, 8, rows), full), vmem),
        (shape((tiles.count, width, 2 * size), low), hbm),
        (shape((2, size, width), low), hbm),
        (shape((grps, slab, both_hidden), low), hbm),
        (shape((grps, units, width), low), hbm),
    ]
    dma = pltpu.SemaphoreType.DMA
    return pl.pallas_call(
        functools.partial(expert_kernel, grps, exps, cap),
        out_shape=[r[0] for r in results],
        in_specs=[smem] + [vmem] * 2 + [hbm] * 6 + [vmem],
        out_specs=[r[1] for r in results],
        scratch_shapes=[
            pltpu.VMEM((members, cap, rows), low),
            pltpu.VMEM((QUAD * slots, 128), full),
            pltpu.VMEM((QUAD * slots, width), low),
            pltpu.VMEM((QUAD * slots, width), low),
            pltpu.VMEM((tiles.count, width, 2 * size), low),
            pltpu.VMEM((tiles.count, size, width), low),
            pltpu.VMEM((2 * exps, rows, width), low),
            pltpu.VMEM((2 * exps, rows, width), low),
            pltpu.VMEM((QUAD * slots, width), low),
            pltpu.VMEM((QUAD * slots, width), low),
            pltpu.VMEM((2, QUAD * slots, 2 * size), low),
            pltpu.VMEM((2, QUAD * slots, size), low),
            [pltpu.VMEM((members >> (1 + step), rows, width), low) for step in range(chip_bits + 1)],
            pltpu.VMEM((members, 8, rows), full),
            pltpu.VMEM((2, rows, width), low),
            dma((2, 2)),
            dma((2, 2)),
            dma((2,)),
            dma((2, 2 * reps)),
            dma((2, reps + 1)),
            dma((2, 2 * reps)),
            dma((2, max(QUAD, grps))),
            dma((2, tiles.count)),
            dma((2, 2, members // 2)),
            dma((2, 3 << chip_bits)),
            dma((2, members)),
        ],
        compiler_params=pltpu.CompilerParams(
            collective_id=2, has_side_effects=True, vmem_limit_bytes=60 * 1024 * 1024
        ),
        name="experts",
    )(deal, routes_t, comb_all, n_all, cot_all, both_w, down_w, in_low, down_slab, h1)


def adamw_root(weight, moment, second, gradient, step_rate, decay_factor):
    new_moment = beta_one * moment + (1.0 - beta_one) * gradient
    new_second = beta_two * second + (1.0 - beta_two) * gradient * gradient
    root = lax.rsqrt(new_second * (1.0 / (1.0 - beta_two**STEP)))
    step = new_moment * (root * (1.0 - eps_adam * root))
    keep = 1.0 - step_rate * decay_factor
    return (new_moment, new_second, keep * weight - (step_rate / (1.0 - beta_one**STEP)) * step)


def adam_kernel(exps, *refs):
    in_parts, down_parts, qkv_grad, out_grad, small = refs[:5]
    states, news, bias_grad = refs[5:26], refs[26:47], refs[47]
    heads = HEADS // exps
    width = small.shape[1]

    def update(i, grad, rate, decay):
        weight, first, second = [state[...] for state in states[3 * i : 3 * i + 3]]
        values = adamw_root(weight, first, second, grad, rate, decay)
        for new, value in zip(news[3 * i : 3 * i + 3], values, strict=True):
            new[...] = value

    def total(parts):
        result = parts[0].astype(full)
        for k in range(1, parts.shape[0]):
            result = result + parts[k].astype(full)
        return result

    @pl.when(pl.program_id(0) == 0)
    def _():
        update(0, qkv_grad[...], 1.5 / math.sqrt(D), 0.1)
        update(1, out_grad[...], 6.0 / math.sqrt(D), 0.1)
        for e in range(exps):
            for h in range(heads):
                bias_grad[e * heads + h : e * heads + h + 1, :] = small[
                    exps + 3 + e : exps + 4 + e, h * 128 : h * 128 + BUCKETS
                ]
        update(2, bias_grad[...], 0.3, 0.0)
        update(3, small[0:exps, :], 1.0 / math.sqrt(D), 0.1)
        update(4, small[exps : exps + 2, :], 0.5, 0.0)

    update(5, total(in_parts), 1.5 / math.sqrt(D), 0.1)
    update(6, total(down_parts), 1.5 / math.sqrt(FF), 0.1)


def adam_call(exps, in_parts, down_parts, qkv_grad, out_grad, small, states):
    steps = 4

    def whole(array):
        return pl.BlockSpec(array.shape, lambda i: (0,) * array.ndim)

    def columns(array):
        block = array.shape[:-1] + (array.shape[-1] // steps,)
        return pl.BlockSpec(block, lambda i: (0,) * (array.ndim - 1) + (i,))

    specs = [whole(state) for state in states[:15]]
    specs += [columns(state) for state in states[15:18]] + [columns(state) for state in states[18:]]
    return pl.pallas_call(
        functools.partial(adam_kernel, exps),
        grid=(steps,),
        in_specs=[columns(in_parts), columns(down_parts), whole(qkv_grad), whole(out_grad), whole(small)] + specs,
        out_specs=specs,
        out_shape=[jax.ShapeDtypeStruct(state.shape, full) for state in states],
        scratch_shapes=[pltpu.VMEM((HEADS, BUCKETS), full)],
        compiler_params=pltpu.CompilerParams(vmem_limit_bytes=60 * 1024 * 1024),
        name="adam",
    )(in_parts, down_parts, qkv_grad, out_grad, small, *states)


def backward_kernel(
    grps,
    exps,
    lengths,
    deal,
    y_half,
    y_far,
    both_g,
    down_g,
    in_before,
    down_before,
    n1_in,
    cot_all,
    routes_t,
    tokens,
    n_total,
    c_in,
    n2_in,
    probs_in,
    h1_from,
    qkv_from,
    pb_from,
    mine_from,
    wqkv_from,
    wout_from,
    gains,
    router_t,
    *rest,
):
    token_grad, block_out, in_parts, down_parts, qkv_grad, out_grad, small_out = rest[:7]
    scratch = rest[7:]
    (
    h1_in,
    qkv,
    pb,
    mine,
    wqkv,
    wout,
    kept,
    y_bufs,
    dh1,
    dz_send,
    dz_all,
    do_send,
    do_in,
    bias_sum,
    dqkv,
    dqkv_t,
    dn1_send,
    dn1_in,
    wq_send,
    og_send,
    mids,
    far_send,
    far_in,
    small_send,
    small_exp,
    small_sum,
    small_rep,
    y_sem,
    load_sem,
    weight_sem,
    down_sem,
    dz_sem,
    do_sem,
    dn1_sem,
    wq_sem,
    og_sem,
    mid_sem,
    far_sem,
    small_sem,
    small2_sem,
    n1_sem,
    operand_sem,
    ) = scratch
    at = Where(grps, exps)
    reps = at.reps
    rows, width = tokens.shape
    heads = HEADS // exps
    head_dim = width // HEADS
    head_cols = heads * head_dim
    block_cols = min(128, head_cols)
    row_block = wqkv.shape[2]
    out_cols = wout.shape[3]
    tiles = Tiles(down_parts.shape[1], reps)
    scale = 1.0 / math.sqrt(head_dim)
    SEND, RECV = 0, 1
    plane = at.quad * exps + at.exp
    members = QUAD * exps

    def exp_peer(k):
        return (at.exp + k) % exps

    router = router_t[...]
    met = greet(*neighbours(at))
    n1 = kept.at[0:exps]
    group = pl.ds(pl.multiple_of(at.quad * exps, exps), exps)
    cot_copy = pltpu.make_async_copy(cot_all.at[group], dn1_send, n1_sem.at[1])
    cot_copy.start()
    loads = [
        pltpu.make_async_copy(src, dst, operand_sem.at[i])
        for i, (src, dst) in enumerate(
            ((h1_from, h1_in), (wout_from, wout), (qkv_from, qkv), (pb_from, pb), (mine_from, mine), (wqkv_from, wqkv))
        )
    ]
    ys = Halving(at, y_bufs, y_sem, [[0, 1, 2], [0, 1, 2], [1, 0, 2]])
    half_loads = [
        pltpu.make_async_copy(y_far, y_bufs[0], load_sem.at[0]),
        pltpu.make_async_copy(y_half, kept, load_sem.at[1]),
    ]
    for copy in loads + half_loads:
        copy.start()

    span = 2 * rows
    met()

    homes = [
        Homeward(
            at,
            tiles,
            t,
            both_g.at[t],
            down_g.at[t - 1] if t else None,
            in_parts,
            down_parts,
            weight_sem.at[t],
            down_sem.at[t],
            (0, 1) if t else (1,),
        )
        for t in range(tiles.count)
    ]
    homes[0].start()
    homes[1].start()
    n1_copy = pltpu.make_async_copy(n1_in, n1, n1_sem.at[0])

    lane = lane_of((rows, 128))
    comb_rows = []
    for e in range(exps):
        total = c_in[e]
        for q in range(1, QUAD):
            total = total + c_in[q * exps + e]
        comb_rows.append(total[0:1, :])
    comb_rows.append(jnp.zeros((128 - exps, rows), full))
    comb_grad = jnp.concatenate(comb_rows, axis=0).T
    valid = row_of((rows, 1)) < lengths[at.me]
    probs = probs_in[...]
    hot = routed(routes_t, at.me, rows)
    picked = jnp.where(hot, probs, 0.0)
    total = jnp.sum(picked, axis=1, keepdims=True)
    gate = picked / total
    gate_grad_rows = jnp.where(valid, comb_grad, 0.0)
    spread_grad = jnp.sum(gate_grad_rows * gate, axis=1, keepdims=True)
    probs_grad = jnp.where(hot, (gate_grad_rows - spread_grad) / total, 0.0)
    logit_grad = probs * (probs_grad - jnp.sum(probs_grad * probs, axis=1, keepdims=True))
    small_rows = small_send.shape[0]
    small_send[...] = jnp.zeros_like(small_send)
    router_back = jnp.dot(
        logit_grad, jnp.concatenate([router, jnp.zeros((128 - exps, width), full)], axis=0),
        precision=highest, preferred_element_type=full,
    )
    for copy in loads:
        copy.wait()
    h1 = h1_in[...]
    r2 = lax.rsqrt(jnp.mean(h1 * h1, axis=1, keepdims=True) + eps_norm)

    steps = len(ys.chip_bits)
    n2_grad = router_back + n_total[...].astype(full)
    scaled = n2_grad * gains[1:2, :]
    cot_copy.wait()
    dealt = deal[at.me] - at.base
    g = dn1_send[0]
    for e in range(1, exps):
        g = jnp.where(dealt == e, dn1_send[e], g)
    hidden_grad = (
        jnp.where(valid, g.astype(full), 0.0)
        + r2 * scaled
        - h1 * (r2 * r2 * r2) * jnp.mean(scaled * h1, axis=1, keepdims=True)
    )
    dh1[...] = hidden_grad
    small_send[exps + 1 : exps + 2, :] = jnp.sum(n2_grad * h1 * r2, axis=0, keepdims=True)
    branch = hidden_grad.astype(low)
    dz_send[...] = branch
    for e in range(exps):
        total = jnp.zeros((rows, row_block), full)
        for r in range(reps):
            total = total + nt(branch[:, r * out_cols : (r + 1) * out_cols], wout[e, r])
        do_send[e] = total.astype(low)

    def do_copies():
        return [
            send(
                do_send.at[exp_peer(k)],
                do_in.at[at.exp],
                do_sem.at[SEND, exp_peer(k)],
                do_sem.at[RECV, at.exp],
                at.device(at.rep, exp_peer(k)),
            )
            for k in range(1, exps)
        ]

    for copy in do_copies():
        copy.start()
    pltpu.make_async_copy(do_send.at[at.exp], do_in.at[at.exp], do_sem.at[RECV, at.exp]).start()

    group_dz = Group(at, dz_send, dz_all, dz_sem)
    dz_all[at.exp] = branch
    for copy in half_loads:
        copy.wait()

    def add_halves(j, _):
        y_bufs[0][j] = y_bufs[0][j] + kept[j]
        return 0

    lax.fori_loop(0, kept.shape[0], add_halves, 0)
    n1_copy.start()

    bias_sum[...] = jnp.zeros_like(bias_sum)

    def dn1_copies():
        beside, across = turn(at.exp, 2), turn(at.exp, 1)
        return [
            functools.partial(
                send, dn1_send.at[k], dn1_in.at[j], dn1_sem.at[SEND, j], dn1_sem.at[RECV, j], at.device(at.rep, to)
            )
            for k, j, to in ((turn(at.exp, 0), 2, beside), (across, 0, across), (beside, 1, beside))
        ]

    def attend_back(i, _):
        s = turn(at.exp, i)
        arrived(do_in.at[s], do_sem.at[RECV, s])

        @pl.when(i == 0)
        def _():
            group_dz.start()
            ys.start(0)

        @pl.when(i == 1)
        def _():
            homes[2].start()

        @pl.when(i == 2)
        def _():
            group_dz.pass_on()

        block_lane = lane_of((rows, block_cols))
        for c in range(head_cols // block_cols):
            cols = slice(c * block_cols, (c + 1) * block_cols)
            k_cols = slice(head_cols + c * block_cols, head_cols + (c + 1) * block_cols)
            v_cols = slice(2 * head_cols + c * block_cols, 2 * head_cols + (c + 1) * block_cols)
            q = qkv[s, :, cols] * scale
            k = qkv[s, :, k_cols]
            v = qkv[s, :, v_cols]
            do = do_in[s, :, cols]
            dq = jnp.zeros((rows, block_cols), full)
            dk = jnp.zeros((rows, block_cols), full)
            dv = jnp.zeros((rows, block_cols), full)
            for t in range(block_cols // head_dim):
                h = c * (block_cols // head_dim) + t
                here = jnp.logical_and(block_lane >= t * head_dim, block_lane < (t + 1) * head_dim)
                zero = jnp.zeros_like(q)
                do_h = jnp.where(here, do, zero)
                weights = pb[s * heads + h]
                p = weights.astype(full)
                dp = nt(do_h, v)
                delta = jnp.sum(dp * p, axis=1, keepdims=True)
                ds = (p * (dp - delta)).astype(low)
                bias_sum[h] += ds.astype(full)
                dv = jnp.where(here, tn(weights, do), dv)
                dq = jnp.where(here, jnp.dot(ds, k, preferred_element_type=full), dq)
                dk = jnp.where(here, tn(ds, q), dk)
            dqkv[:, cols] = (dq * scale).astype(low)
            dqkv[:, k_cols] = dk.astype(low)
            dqkv[:, v_cols] = dv.astype(low)
        dqkv_t[:, pl.ds(pl.multiple_of(s * rows, rows), rows)] = dqkv[...].T
        for e in range(exps):
            dn1_send[s, :, e * row_block : (e + 1) * row_block] = jnp.dot(
                dqkv[...], wqkv[e], preferred_element_type=full
            ).astype(low)

        @pl.when(i == 0)
        def _():
            dn1_copies()[0]().start()

        @pl.when(i == 1)
        def _():
            arrived(dn1_in.at[2], dn1_sem.at[RECV, 2])
            dn1_send[s] = (dn1_send[s].astype(full) + dn1_in[2].astype(full)).astype(low)
            dn1_copies()[1]().start()

        @pl.when(i == 2)
        def _():
            dn1_copies()[2]().start()

        return 0

    lax.fori_loop(0, exps, attend_back, 0)
    ys.next(0)

    n1_copy.wait()
    seg = wq_send.shape[2]
    parts = wq_send.shape[1]
    segs = mids.shape[1] - 1
    for e in range(exps):
        part = kept[0:exps, :, e * row_block : (e + 1) * row_block].reshape(exps * rows, row_block)
        total = dot(dqkv_t[...], part)
        for j in range(parts):
            wq_send[e, j] = total[j * seg : (j + 1) * seg].astype(low)

    def owner(j):
        section, within = j // (head_cols // seg), j % (head_cols // seg)
        col = section * width + at.exp * head_cols + within * seg
        block = col // seg
        return block // segs, block % segs

    def mid_place(grp, k, quad):
        return (grp * (segs + 1) + k) * QUAD + quad

    def mid_copy(src, send_sem, rep, k, e):
        dst = mids.at[rep // QUAD, k, at.quad]
        recv = mid_sem.at[mid_place(rep // QUAD, k, at.quad)]
        stays = jnp.logical_and(rep % QUAD == at.quad, e == at.exp)
        return (
            stays,
            functools.partial(send, src, dst, send_sem, recv, (at.grp, rep % QUAD, e)),
            functools.partial(pltpu.make_async_copy, src, dst, recv),
        )

    def wq_copy(i):
        e, j = i // parts, i % parts
        rep, k = owner(j)
        return mid_copy(wq_send.at[e, j], wq_sem.at[i], rep, k, e)

    def og_copy(r):
        return mid_copy(og_send.at[r], og_sem.at[r], r, segs, at.exp)

    def go(copies, act, act_local):
        stays, away, local = copies

        @pl.when(jnp.logical_not(stays))
        def _():
            act(away)

        if act_local:

            @pl.when(stays)
            def _():
                act_local(local)

    def over(count, copies, act, act_local):
        def one(i, _):
            go(copies(i), act, act_local)
            return 0

        lax.fori_loop(0, count, one, 0)

    over(exps * parts, wq_copy, lambda copy: copy().start(), lambda copy: copy().start())
    group_dz.arrive()
    grad = tn(mine[...].reshape(exps * rows, head_cols), dz_all[...].reshape(exps * rows, width))
    for r in range(reps):
        og_send[r] = grad[:, r * out_cols : (r + 1) * out_cols].T.astype(low)
    over(reps, og_copy, lambda copy: copy().start(), lambda copy: copy().start())

    n1_grad = dn1_send[at.exp].astype(full)
    for j in range(2):
        arrived(dn1_in.at[j], dn1_sem.at[RECV, j])
        n1_grad = n1_grad + dn1_in[j].astype(full)
    x = tokens[...].astype(full)
    r1 = lax.rsqrt(jnp.mean(x * x, axis=1, keepdims=True) + eps_norm)
    scaled = n1_grad * gains[0:1, :]
    token_grad[...] = (
        dh1[...] + r1 * scaled - x * (r1 * r1 * r1) * jnp.mean(scaled * x, axis=1, keepdims=True)
    )
    small_send[exps : exps + 1, :] = jnp.sum(n1_grad * x * r1, axis=0, keepdims=True)

    ys.next(1)
    router_rows = lax.dot_general(
        logit_grad, n2_in[...].astype(full), (((0,), (0,)), ((), ())), preferred_element_type=full, precision=highest
    )
    small_send[0:exps, :] = router_rows[0:exps, :]

    flip = jnp.where(row_of((rows, rows)) + lane_of((rows, rows)) == rows - 1, 1.0, 0.0).astype(low)
    diagonals = []
    for h in range(heads):
        high = bias_sum[h].astype(low)
        rest = (bias_sum[h] - high.astype(full)).astype(low)
        flipped = dot(high, flip) + dot(rest, flip)
        square = jnp.concatenate([flipped, jnp.zeros((rows, rows), full)], axis=1)
        turned = pltpu.roll(square, 0, 1, stride=1, stride_axis=0)
        diagonals.append(jnp.sum(turned, axis=0, keepdims=True))
    diagonals = jnp.concatenate(diagonals + [jnp.zeros((8 - heads, span), full)], axis=0)
    in_bucket = jnp.where(bucket_of(rows - 1 - row_of((span, 128))) == lane_of((span, 128)), 1.0, 0.0)
    bias_line = jnp.dot(diagonals, in_bucket, precision=highest, preferred_element_type=full)
    for h in range(heads):
        small_send[exps + 2 : exps + 3, h * 128 : (h + 1) * 128] = bias_line[h : h + 1, :]

    def small_copies():
        return [
            send(
                small_send,
                small_exp.at[at.exp],
                small_sem.at[SEND, exp_peer(k)],
                small_sem.at[RECV, at.exp],
                at.device(at.rep, exp_peer(k)),
            )
            for k in range(1, exps)
        ]

    for copy in small_copies():
        copy.start()
    small_exp[at.exp] = small_send[...]

    def mid_sum(grp, k):
        for q in range(QUAD):
            arrived(mids.at[grp, k, q], mid_sem.at[mid_place(grp, k, q)])
        total = mids[grp, k, 0].astype(full)
        for q in range(1, QUAD):
            total = total + mids[grp, k, q].astype(full)
        return total

    far = 1 - at.grp
    for k in range(segs + 1):
        far_send[k] = mid_sum(far, k).astype(low)

    def far_copy():
        return send(far_send, far_in, far_sem.at[SEND], far_sem.at[RECV], (far, at.quad, at.exp))

    far_copy().start()
    for k in range(1, exps):
        arrived(small_exp.at[exp_peer(k)], small_sem.at[RECV, exp_peer(k)])
    total = small_exp[0]
    for e in range(1, exps):
        total = total + small_exp[e]
    small_sum[0] = total
    for e in range(exps):
        small_sum[0, exps + 3 + e : exps + 4 + e, :] = small_exp[e, exps + 2 : exps + 3, :]

    def small2_copies():
        return [
            send(
                small_sum.at[0],
                small_rep.at[at.rep],
                small2_sem.at[SEND, (at.rep + k) % reps],
                small2_sem.at[RECV, at.rep],
                at.device((at.rep + k) % reps, at.exp),
            )
            for k in range(1, reps)
        ]

    for copy in small2_copies():
        copy.start()
    small_rep[at.rep] = small_sum[0]
    for step in range(2, steps):
        ys.next(step)
    length = lengths[at.base]
    for e in range(1, exps):
        length = jnp.where(deal[at.base + e] == at.me, lengths[at.base + e], length)
    block = ys.result()[0]
    block_out[...] = jnp.where(row_of((rows, 1)) < length, block, jnp.zeros_like(block))
    for k in range(1, reps):
        arrived(small_rep.at[(at.rep + k) % reps], small2_sem.at[RECV, (at.rep + k) % reps])
    total = small_rep[0]
    for r in range(1, reps):
        total = total + small_rep[r]
    small_out[...] = total

    near = [mid_sum(at.grp, k) for k in range(segs + 1)]
    arrived(far_in, far_sem.at[RECV])
    grads = [(near[k] + far_in[k].astype(full)).T for k in range(segs + 1)]
    qkv_grad[...] = jnp.concatenate(grads[:segs], axis=1)
    out_grad[...] = grads[segs]
    for home in homes:
        home.arrive()

    ys.finish()

    for home in homes:
        home.sent()

    over(exps * parts, wq_copy, lambda copy: copy().wait_send(), None)
    over(reps, og_copy, lambda copy: copy().wait_send(), None)
    far_copy().wait_send()
    for copies in (do_copies(), small_copies(), small2_copies()):
        for copy in copies:
            copy.wait_send()
    for copy in dn1_copies():
        copy().wait_send()
    group_dz.sent()


def routed(routes_t, seq, rows):
    pair = routes_t[:, pl.ds(pl.multiple_of(seq * rows, rows), rows)].astype(full)
    cols = jnp.concatenate([pair, jnp.zeros((126, rows), full)], axis=0).T
    lane = lane_of((rows, 128)).astype(full)
    return jnp.logical_or(lane == cols[:, 0:1], lane == cols[:, 1:2])


def backward_call(
    grps, exps, lengths, deal, y_half, y_far, both_g, down_g, in_before, down_before, n1,
    cot_all, routes_t, tokens, n_total, c_in, n2, probs, h1, qkv, pb, mine, wqkv, wout, gains, router
):
    reps = grps * QUAD
    rows, width = tokens.shape
    heads = HEADS // exps
    head_cols = width // exps
    row_block = wqkv.shape[2]
    out_cols = wout.shape[3]
    shard_cols = 3 * width // reps
    seg = math.gcd(shard_cols, head_cols)
    segs = shard_cols // seg
    parts = 3 * head_cols // seg
    members = QUAD * exps
    chip_bits = bits_of(members) - 1
    small_rows = -(-(2 * exps + 3) // 8) * 8
    shape = jax.ShapeDtypeStruct
    vmem = pl.BlockSpec(memory_space=pltpu.VMEM)
    smem = pl.BlockSpec(memory_space=pltpu.SMEM)
    hbm = pl.BlockSpec(memory_space=pl.ANY)
    results = [
        (shape((rows, width), full), vmem),
        (shape((rows, width), low), vmem),
        (shape(in_before.shape, low), hbm),
        (shape(down_before.shape, low), hbm),
        (shape((row_block, shard_cols), full), vmem),
        (shape((row_block, out_cols), full), vmem),
        (shape((small_rows, width), full), vmem),
    ]
    dma = pltpu.SemaphoreType.DMA
    bufs = [pltpu.VMEM((1 << (chip_bits - s), rows, width), low) for s in range(chip_bits + 1)]
    return pl.pallas_call(
        functools.partial(backward_kernel, grps, exps),
        out_shape=[r[0] for r in results],
        in_specs=[smem] * 2 + [hbm] * 8 + [vmem] * 6 + [hbm] * 6 + [vmem] * 2,
        out_specs=[r[1] for r in results],
        scratch_shapes=[
            pltpu.VMEM(h1.shape, full),
            pltpu.VMEM(qkv.shape, low),
            pltpu.VMEM(pb.shape, low),
            pltpu.VMEM(mine.shape, low),
            pltpu.VMEM(wqkv.shape, low),
            pltpu.VMEM(wout.shape, low),
            pltpu.VMEM((members // 2, rows, width), low),
            list(bufs),
            pltpu.VMEM((rows, width), full),
            pltpu.VMEM((rows, width), low),
            pltpu.VMEM((exps, rows, width), low),
            pltpu.VMEM((exps, rows, head_cols), low),
            pltpu.VMEM((exps, rows, head_cols), low),
            pltpu.VMEM((heads, rows, rows), full),
            pltpu.VMEM((rows, 3 * head_cols), low),
            pltpu.VMEM((3 * head_cols, exps * rows), low),
            pltpu.VMEM((exps, rows, width), low),
            pltpu.VMEM((3, rows, width), low),
            pltpu.VMEM((exps, parts, seg, row_block), low),
            pltpu.VMEM((reps, seg, row_block), low),
            pltpu.VMEM((grps, segs + 1, QUAD, seg, row_block), low),
            pltpu.VMEM((segs + 1, seg, row_block), low),
            pltpu.VMEM((segs + 1, seg, row_block), low),
            pltpu.VMEM((small_rows, width), full),
            pltpu.VMEM((exps, small_rows, width), full),
            pltpu.VMEM((1, small_rows, width), full),
            pltpu.VMEM((reps, small_rows, width), full),
            dma((2, 3 << chip_bits)),
            dma((2,)),
            dma((3, 2, 2 * reps)),
            dma((3, 2, max(QUAD, grps))),
            dma((2, exps)),
            dma((2, exps)),
            dma((2, exps)),
            dma((exps * parts,)),
            dma((reps,)),
            dma((grps * (segs + 1) * QUAD,)),
            dma((2,)),
            dma((2, exps)),
            dma((2, reps)),
            dma((2,)),
            dma((6,)),
        ],
        compiler_params=pltpu.CompilerParams(
            collective_id=1, has_side_effects=True, vmem_limit_bytes=60 * 1024 * 1024
        ),
        input_output_aliases={6: 2, 7: 3},
        name="backward",
    )(
        lengths, deal, y_half, y_far, both_g, down_g, in_before, down_before, n1, cot_all,
        routes_t, tokens, n_total, c_in, n2, probs, h1, qkv, pb, mine, wqkv, wout, gains, router
    )


def per_device(
    tokens,
    cotangent,
    seq_lengths,
    deal,
    routes,
    attn_qkv,
    qkv_first,
    qkv_second,
    attn_out,
    out_first,
    out_second,
    rel_bias,
    bias_first,
    bias_second,
    router,
    router_first,
    router_second,
    norm_gains,
    gains_first,
    gains_second,
    expert_in,
    in_first,
    in_second,
    expert_out,
    down_first,
    down_second,
):
    rows, width = tokens.shape
    experts = router.shape[1]
    capacity = (10 * rows + 4 * experts - 1) // (4 * experts)
    exps = lax.axis_size("exp")
    grps = lax.axis_size("grp")
    routes_t = routes.T
    bias_table = rel_bias.T
    (
        both_w, down_w, cot_all, n_all, comb_all, qkv, pb, context_mine, normed_group, wqkv, wout, hidden_one,
        normed_two, router_probs, in_low, down_low,
    ) = forward_call(
        grps, exps, seq_lengths, bias_table, routes_t, tokens, cotangent, norm_gains.T, router.T,
        attn_qkv, attn_out, expert_in[0], expert_out[0],
    )
    n_total, y_half, y_far, c_in, both_g, down_g, in_before, down_before = expert_call(
        grps, exps, capacity, deal, routes_t, comb_all, n_all, cot_all, both_w, down_w, in_low, down_low,
        hidden_one,
    )
    token_grad, block_out, in_parts, down_parts, qkv_grad, out_grad, small = backward_call(
        grps, exps, seq_lengths, deal, y_half, y_far, both_g, down_g,
        in_before, down_before, normed_group, cot_all, routes_t, tokens, n_total, c_in, normed_two, router_probs, hidden_one, qkv, pb, context_mine, wqkv,
        wout, norm_gains.T, router.T,
    )
    states = [
        attn_qkv, qkv_first, qkv_second, attn_out, out_first, out_second, bias_table, bias_first.T, bias_second.T,
        router.T, router_first.T, router_second.T, norm_gains.T, gains_first.T, gains_second.T,
        expert_in[0], in_first[0], in_second[0], expert_out[0], down_first[0], down_second[0],
    ]
    new = list(adam_call(exps, in_parts, down_parts, qkv_grad, out_grad, small, states))
    new = new[:6] + [array.T for array in new[6:15]] + [array[None] for array in new[15:]]
    return (block_out, token_grad, *new)


def bucket_onehot(length):
    places = jnp.arange(length, dtype=jnp.int32)
    offset = places[None, :] - places[:, None]
    distance = jnp.abs(offset)
    bucket = 16 * (offset > 0).astype(jnp.int32)
    for threshold in thresholds:
        bucket = bucket + (distance >= threshold).astype(jnp.int32)
    return (bucket[:, :, None] == jnp.arange(BUCKETS, dtype=jnp.int32)[None, None, :]).astype(full)


def swap(pieces, axes):
    return lax.all_to_all(pieces, axes, split_axis=0, concat_axis=0, tiled=True)


def spread(block, axes):
    members = lax.axis_size(axes)
    return swap(jnp.broadcast_to(block[None], (members,) + block.shape), axes)


def plain_device(
    tokens,
    cotangent,
    seq_lengths,
    deal,
    routes,
    attn_qkv,
    qkv_first,
    qkv_second,
    attn_out,
    out_first,
    out_second,
    rel_bias,
    bias_first,
    bias_second,
    router,
    router_first,
    router_second,
    norm_gains,
    gains_first,
    gains_second,
    expert_in,
    in_first,
    in_second,
    expert_out,
    down_first,
    down_second,
):
    rows, width = tokens.shape
    head_dim = width // HEADS
    score_scale = 1.0 / math.sqrt(head_dim)
    experts = router.shape[1]
    capacity = (10 * rows + 4 * experts - 1) // (4 * experts)
    exps = lax.axis_size("exp")
    grps = lax.axis_size("grp")
    reps = grps * QUAD
    heads = HEADS // exps
    head_cols = heads * head_dim
    place = lax.axis_index("exp")
    base = lax.axis_index(REP) * exps
    me = base + place
    slab = expert_in.shape[1]
    units = expert_out.shape[1]
    quarter = grps * units

    row_block = attn_qkv.shape[0]
    qkv_rows = lax.all_gather(attn_qkv.astype(low), REP, axis=1, tiled=True)
    out_rows = lax.all_gather(attn_out.astype(low), REP, axis=1, tiled=True)
    qkv_pieces = jnp.transpose(
        qkv_rows.reshape(row_block, 3, exps, head_cols), (2, 0, 1, 3)
    ).reshape(exps, row_block, 3 * head_cols)
    qkv_mine = swap(qkv_pieces, "exp").reshape(width, 3 * head_cols)
    full_out = spread(out_rows, "exp").reshape(width, width)

    group_tokens = spread(tokens, "exp")
    group_cotangent = spread(cotangent, "exp")
    my_cotangent = lax.dynamic_index_in_dim(group_cotangent, deal[me] - base, 0, keepdims=False)

    my_routes = lax.dynamic_slice_in_dim(routes, me * rows, rows, 0)
    places = jnp.arange(rows, dtype=jnp.int32)
    valid_rows = (places < seq_lengths[me]).astype(full)
    group_lengths = lax.dynamic_slice_in_dim(seq_lengths, base, exps, 0)
    key_ok = places[None, :] < group_lengths[:, None]
    gain_one = norm_gains[:, 0]
    gain_two = norm_gains[:, 1]

    chosen = (my_routes[:, :, None] == jnp.arange(experts, dtype=jnp.int32)[None, None, :]).astype(full)
    flat_routes = my_routes.reshape(-1)
    route_hot = (flat_routes[:, None] == jnp.arange(experts, dtype=jnp.int32)[None, :]).astype(jnp.int32)
    before = jnp.cumsum(route_hot, axis=0) - route_hot
    slot_index = jnp.sum(before * route_hot, axis=-1)
    target = (flat_routes * capacity + slot_index).reshape(rows, 2)
    slots = experts * capacity
    slot_ids = jnp.arange(slots, dtype=jnp.int32)
    place_first = slot_ids[:, None] == target[None, :, 0]
    place_second = slot_ids[:, None] == target[None, :, 1]
    place_any = jnp.logical_or(place_first, place_second).astype(low)

    shard_in = expert_in[0].astype(low).reshape(slab, 2, grps, QUAD, units)
    in_pieces = jnp.transpose(shard_in, (1, 3, 0, 2, 4)).reshape(2, 1, QUAD, slab, quarter)
    in_pieces = jnp.broadcast_to(in_pieces, (2, grps, QUAD, slab, quarter)).reshape(
        2, reps, slab, quarter
    )
    down_mine = spread(expert_out[0].astype(low), "grp").reshape(quarter, width)
    gate_mine = swap(in_pieces[0], REP).reshape(width, quarter)
    up_mine = swap(in_pieces[1], REP).reshape(width, quarter)

    upstream = my_cotangent.astype(full) * valid_rows[:, None]

    def to_experts(block):
        sent = block.reshape((1, experts) + block.shape[1:])
        sent = jnp.broadcast_to(sent, (QUAD,) + sent.shape[1:])
        return swap(sent.reshape((QUAD * experts,) + block.shape[1:]), PLANE)

    def dispatch(values):
        return dot(place_any, values).astype(low).reshape(experts, capacity, width)

    expert_upstream = to_experts(dispatch(upstream.astype(low))).reshape(-1, width)
    active_grad_bare = lax.dot_general(
        expert_upstream, down_mine, (((1,), (1,)), ((), ())), preferred_element_type=full
    )

    x_group = group_tokens.astype(full)
    scale_group = lax.rsqrt(jnp.mean(x_group * x_group, axis=-1, keepdims=True) + eps_norm)
    normed_group = (x_group * scale_group * gain_one).astype(low).reshape(exps * rows, width)
    qkv = dot(normed_group, qkv_mine).astype(low).reshape(exps, rows, 3, heads, head_dim)
    queries = qkv[:, :, 0]
    key_rows = qkv[:, :, 1]
    values = qkv[:, :, 2]
    onehot = bucket_onehot(rows)
    bias_mine = lax.dynamic_slice_in_dim(rel_bias, place * heads, heads, 1)
    bias_table = jnp.einsum("ijb,bh->hij", onehot, bias_mine, precision=highest)

    def scores_of():
        raw = (
            jnp.einsum("sihd,sjhd->shij", queries, key_rows, preferred_element_type=full)
            * score_scale
            + bias_table[None]
        )
        return jnp.where(key_ok[:, None, None, :], raw, -1e30)

    scores = scores_of()
    row_max = jnp.max(scores, axis=-1, keepdims=True)
    log_total = row_max + jnp.log(jnp.sum(jnp.exp(scores - row_max), axis=-1, keepdims=True))
    weights_low = jnp.exp(scores - log_total).astype(low)
    context_mine = (
        jnp.einsum("shij,sjhd->sihd", weights_low, values, preferred_element_type=full)
        .astype(low)
        .reshape(exps, rows, head_cols)
    )
    context = jnp.transpose(swap(context_mine, "exp"), (1, 0, 2)).reshape(rows, width)

    x_float = tokens.astype(full)
    scale_one = lax.rsqrt(jnp.mean(x_float * x_float, axis=-1, keepdims=True) + eps_norm)
    hidden_one = x_float + dot(context, full_out)
    scale_two = lax.rsqrt(jnp.mean(hidden_one * hidden_one, axis=-1, keepdims=True) + eps_norm)
    normed_two = (hidden_one * scale_two * gain_two).astype(low)
    normed_float = normed_two.astype(full)
    router_probs = jax.nn.softmax(jnp.dot(normed_float, router, precision=highest), axis=-1)
    picked = jnp.sum(router_probs[:, None, :] * chosen, axis=-1)
    gate_total = jnp.sum(picked, axis=-1, keepdims=True)
    gate_value = picked / gate_total
    combine = gate_value * valid_rows[:, None]
    combine_slots = jnp.sum(
        jnp.where(place_first, combine[None, :, 0], 0.0)
        + jnp.where(place_second, combine[None, :, 1], 0.0),
        axis=1,
    ).reshape(experts, 1, capacity)

    expert_rows = to_experts(dispatch(normed_two)).reshape(-1, width)
    expert_combine = to_experts(combine_slots).reshape(-1, 1)

    gate_part = dot(expert_rows, gate_mine)
    up_part = dot(expert_rows, up_mine)
    active_float, active_pull = jax.vjp(gated_unit, gate_part, up_part)
    active = active_float.astype(low)
    active_scaled = (active_float * expert_combine).astype(low)
    combine_grad_part = jnp.sum(active_float * active_grad_bare, axis=-1).reshape(
        QUAD * experts, 1, capacity
    )
    gate_part_grad, up_part_grad = active_pull(active_grad_bare * expert_combine)
    gate_part_grad = gate_part_grad.astype(low)
    up_part_grad = up_part_grad.astype(low)
    rows_grad_part = (
        lax.dot_general(gate_part_grad, gate_mine, (((1,), (1,)), ((), ())), preferred_element_type=full)
        + lax.dot_general(up_part_grad, up_mine, (((1,), (1,)), ((), ())), preferred_element_type=full)
    ).astype(low)
    output_part = dot(active, down_mine).astype(low)

    combine_grad_back = swap(combine_grad_part, PLANE)
    rows_grad_back = swap(rows_grad_part.reshape(QUAD * experts, capacity, width), PLANE)
    output_back = swap(output_part.reshape(QUAD * experts, capacity, width), PLANE)

    def transposed_dot(a, b):
        return lax.dot_general(a, b, (((0,), (0,)), ((), ())), preferred_element_type=full)

    down_grad = transposed_dot(active_scaled, expert_upstream).astype(low)
    gate_grad = transposed_dot(expert_rows, gate_part_grad).astype(low)
    up_grad = transposed_dot(expert_rows, up_part_grad).astype(low)
    down_share = jnp.sum(
        swap(down_grad.reshape(grps, units, width), "grp").astype(full), axis=0
    )[None]

    def in_columns(grad):
        back = swap(grad.reshape(reps, slab, quarter), REP).astype(full)
        back = jnp.sum(back.reshape(grps, QUAD, slab, grps, units), axis=0)
        return jnp.transpose(back, (1, 2, 0, 3)).reshape(slab, grps * QUAD * units)

    in_share = jnp.concatenate([in_columns(gate_grad), in_columns(up_grad)], axis=1)[None]

    def from_slots(placed, parts):
        hot = jnp.broadcast_to(placed.astype(low)[None], (QUAD,) + placed.shape).reshape(-1, rows)
        return lax.dot_general(
            hot, parts.reshape(-1, width), (((0,), (0,)), ((), ())), preferred_element_type=full
        )

    mixture = combine[:, :1] * from_slots(place_first, output_back) + combine[:, 1:] * from_slots(
        place_second, output_back
    )
    block_loader = (valid_rows[:, None] * (hidden_one + mixture)).astype(low)
    seq_ids = jnp.arange(deal.shape[0], dtype=jnp.int32)
    dealt_seq = jnp.sum(jnp.where(deal == me, seq_ids, 0))
    block_out = lax.dynamic_index_in_dim(
        spread(block_loader, "exp"), dealt_seq - base, 0, keepdims=False
    )

    combine_grad_slots = jnp.sum(combine_grad_back.reshape(QUAD, slots), axis=0)
    combine_grad = jnp.stack(
        [
            jnp.sum(jnp.where(place_first, combine_grad_slots[:, None], 0.0), axis=0),
            jnp.sum(jnp.where(place_second, combine_grad_slots[:, None], 0.0), axis=0),
        ],
        axis=1,
    )
    gate_grad_value = combine_grad * valid_rows[:, None]
    picked_grad = (
        gate_grad_value - jnp.sum(gate_grad_value * gate_value, axis=-1, keepdims=True)
    ) / gate_total
    probs_grad = jnp.sum(picked_grad[:, :, None] * chosen, axis=1)
    logit_grad = router_probs * (
        probs_grad - jnp.sum(probs_grad * router_probs, axis=-1, keepdims=True)
    )
    router_grad = jnp.dot(normed_float.T, logit_grad, precision=highest)
    normed_grad = jnp.dot(logit_grad, router.T, precision=highest) + from_slots(
        jnp.logical_or(place_first, place_second), rows_grad_back
    )
    scaled_two = normed_grad * gain_two
    hidden_grad = (
        upstream
        + scale_two * scaled_two
        - hidden_one * scale_two**3 * jnp.mean(scaled_two * hidden_one, axis=-1, keepdims=True)
    )
    gain_two_grad = jnp.sum(normed_grad * hidden_one * scale_two, axis=0)
    branch_grad = hidden_grad.astype(low)
    context_grad = lax.dot_general(
        branch_grad, full_out, (((1,), (1,)), ((), ())), preferred_element_type=full
    ).astype(low)
    context_grad_pieces = jnp.transpose(context_grad.reshape(rows, exps, head_cols), (1, 0, 2))
    context_grad_mine = swap(context_grad_pieces, "exp").reshape(exps, rows, heads, head_dim)
    branch_group = spread(branch_grad, "exp").reshape(exps * rows, width)
    out_grad = transposed_dot(context_mine.reshape(exps * rows, head_cols), branch_group).astype(low)

    scores = scores_of()
    probs_again = jnp.exp(scores - log_total)
    weights_again = probs_again.astype(low)
    values_grad = jnp.einsum(
        "shij,sihd->sjhd", weights_again, context_grad_mine, preferred_element_type=full
    )
    probs_grad_att = jnp.einsum(
        "sihd,sjhd->shij", context_grad_mine, values, preferred_element_type=full
    )
    row_delta = jnp.sum(probs_grad_att * probs_again, axis=-1, keepdims=True)
    scores_grad = (probs_again * (probs_grad_att - row_delta)).astype(low)
    scores_grad_sum = jnp.sum(scores_grad.astype(full), axis=0)
    bias_grad_mine = jnp.einsum("hij,ijb->bh", scores_grad_sum, onehot, precision=highest)
    bias_grad = lax.dynamic_update_slice_in_dim(
        jnp.zeros((BUCKETS, HEADS), full), bias_grad_mine, place * heads, 1
    )
    queries_grad = (
        jnp.einsum("shij,sjhd->sihd", scores_grad, key_rows, preferred_element_type=full)
        * score_scale
    )
    keys_grad = (
        jnp.einsum("shij,sihd->sjhd", scores_grad, queries, preferred_element_type=full)
        * score_scale
    )
    qkv_grad = (
        jnp.stack([queries_grad, keys_grad, values_grad], axis=2)
        .astype(low)
        .reshape(exps * rows, 3 * head_cols)
    )
    normed_one_part = lax.dot_general(
        qkv_grad, qkv_mine, (((1,), (1,)), ((), ())), preferred_element_type=full
    ).astype(low)
    normed_one_grad = jnp.sum(
        swap(normed_one_part.reshape(exps, rows, width), "exp").astype(full), axis=0
    )
    scaled_one = normed_one_grad * gain_one
    token_grad = (
        hidden_grad
        + scale_one * scaled_one
        - x_float * scale_one**3 * jnp.mean(scaled_one * x_float, axis=-1, keepdims=True)
    )
    gain_one_grad = jnp.sum(normed_one_grad * x_float * scale_one, axis=0)

    qkv_weight_grad = transposed_dot(normed_group, qkv_grad).astype(low)
    qkv_grad_rows = swap(qkv_weight_grad.reshape(exps, row_block, 3 * head_cols), "exp")
    qkv_grad_rows = jnp.transpose(
        qkv_grad_rows.reshape(exps, row_block, 3, head_cols), (1, 2, 0, 3)
    ).reshape(row_block, reps, -1)
    qkv_share = jnp.sum(
        swap(jnp.transpose(qkv_grad_rows, (1, 0, 2)), REP).astype(full), axis=0
    )
    out_pieces = jnp.transpose(out_grad.reshape(row_block, reps, -1), (1, 0, 2))
    out_share = jnp.sum(swap(out_pieces, REP).astype(full), axis=0)

    small = jnp.concatenate(
        [
            router_grad.reshape(-1),
            jnp.stack([gain_one_grad, gain_two_grad], axis=1).reshape(-1),
            bias_grad.reshape(-1),
        ]
    ).reshape(-1, 128)
    small_total = jnp.sum(lax.all_gather(small, ALL, axis=0, tiled=False), axis=0).reshape(-1)
    router_total = small_total[: router.size].reshape(router.shape)
    gains_total = small_total[router.size : router.size + norm_gains.size].reshape(norm_gains.shape)
    bias_total = small_total[router.size + norm_gains.size :].reshape(rel_bias.shape)

    qkv_new = adamw_update(attn_qkv, qkv_first, qkv_second, qkv_share, 1.5 / math.sqrt(D), 0.1)
    out_new = adamw_update(attn_out, out_first, out_second, out_share, 6.0 / math.sqrt(D), 0.1)
    bias_new = adamw_update(rel_bias, bias_first, bias_second, bias_total, 0.3, 0.0)
    router_new = adamw_update(
        router, router_first, router_second, router_total, 1.0 / math.sqrt(D), 0.1
    )
    gains_new = adamw_update(norm_gains, gains_first, gains_second, gains_total, 0.5, 0.0)
    in_new = adamw_update(expert_in, in_first, in_second, in_share, 1.5 / math.sqrt(D), 0.1)
    down_new = adamw_update(
        expert_out, down_first, down_second, down_share, 1.5 / math.sqrt(FF), 0.1
    )
    return (
        (block_out, token_grad)
        + qkv_new
        + out_new
        + bias_new
        + router_new
        + gains_new
        + in_new
        + down_new
    )


def solution(mesh):
    reps, exps = mesh.devices.shape
    split = Mesh(mesh.devices.reshape(reps // QUAD, QUAD, exps), ALL)
    by_rows = P(ALL, None)
    attn = P("exp", REP)
    expert = P("exp", REP, None)
    return jax.shard_map(
        per_device if (reps, exps) == (2 * QUAD, 4) else plain_device,
        mesh=split,
        in_specs=(by_rows, by_rows) + (P(),) * 3 + (attn,) * 6 + (P(),) * 9 + (expert,) * 6,
        out_specs=(by_rows, by_rows) + (attn,) * 6 + (P(),) * 9 + (expert,) * 6,
        check_vma=False,
    )
```

```python
import functools
import math

import jax
import jax.numpy as jnp
from jax import lax
from jax.experimental import pallas as pl
from jax.experimental.pallas import tpu as pltpu
from jax.sharding import Mesh
from jax.sharding import PartitionSpec as P

D = 1024
HEADS = 16
FF = 2816
BUCKETS = 32
STEP = 10
QUAD = 4
REP = ("grp", "quad")
PLANE = ("quad", "exp")
ALL = ("grp", "quad", "exp")

highest = lax.Precision.HIGHEST
eps_norm = 1e-06
thresholds = (1, 2, 3, 4, 5, 6, 7, 8, 11, 16, 22, 32, 45, 64, 90)
beta_one = 0.9
beta_two = 0.999
eps_adam = 1e-08
low = jnp.bfloat16
full = jnp.float32
MESH = pl.DeviceIdType.MESH


def adamw_update(weight, moment, second, gradient, step_rate, decay_factor):
    new_moment = beta_one * moment + (1.0 - beta_one) * gradient
    new_second = beta_two * second + (1.0 - beta_two) * gradient * gradient
    corrected = new_moment / (1.0 - beta_one**STEP)
    scaled = new_second / (1.0 - beta_two**STEP)
    new_weight = weight - step_rate * (
        corrected / (jnp.sqrt(scaled) + eps_adam) + decay_factor * weight
    )
    return (new_moment, new_second, new_weight)


def gated_unit(gate_input, up_input):
    return jax.nn.gelu(gate_input, approximate=True) * up_input


def dot(a, b):
    return jnp.dot(a, b, preferred_element_type=full)


def nt(a, b, precision=None):
    return lax.dot_general(a, b, (((1,), (1,)), ((), ())), preferred_element_type=full, precision=precision)


def tn(a, b):
    return lax.dot_general(a, b, (((0,), (0,)), ((), ())), preferred_element_type=full)


class Where:
    def __init__(self, grps, exps):
        self.grps, self.exps = grps, exps
        self.reps = grps * QUAD
        self.grp = lax.axis_index("grp")
        self.quad = lax.axis_index("quad")
        self.exp = lax.axis_index("exp")
        self.rep = self.grp * QUAD + self.quad
        self.base = self.rep * exps
        self.me = self.base + self.exp

    def device(self, rep, exp):
        return (rep // QUAD, rep % QUAD, exp)

    def near(self, flip):
        q = self.quad
        if flip & 1:
            q = q + 1 - 2 * (q % 2)
        if flip & 2:
            q = q + 2 - 4 * (q // 2)
        return q


def send(src, dst, send_sem, recv_sem, device):
    return pltpu.make_async_remote_copy(
        src_ref=src, dst_ref=dst, send_sem=send_sem, recv_sem=recv_sem, device_id=device, device_id_type=MESH
    )


def arrived(ref, sem):
    pltpu.make_async_copy(ref, ref, sem).wait()


def greet(count, device):
    barrier = pltpu.get_barrier_semaphore()

    def one(k, _):
        pl.semaphore_signal(barrier, inc=1, device_id=device(k), device_id_type=MESH)
        return 0

    lax.fori_loop(1, count + 1, one, 0)
    return functools.partial(pl.semaphore_wait, barrier, count)


def everyone(at):
    count = at.reps * at.exps

    def device(k):
        other = (at.me + k) % count
        return at.device(other // at.exps, other % at.exps)

    return count - 1, device


def neighbours(at):
    members = QUAD * at.exps
    plane = at.quad * at.exps + at.exp

    def device(k):
        other = (plane + k) % members
        rest = k - members
        grp = jnp.where(k < members, at.grp, (at.grp + 1 + rest // QUAD) % at.grps)
        quad = jnp.where(k < members, other // at.exps, rest % QUAD)
        return grp, quad, jnp.where(k < members, other % at.exps, at.exp)

    return members - 1 + QUAD * (at.grps - 1), device


def turn(exp, i):
    beside = exp + 1 - 2 * (exp % 2)
    return jnp.where(i == 0, (beside + 2) % 4, jnp.where(i == 1, (exp + 2) % 4, jnp.where(i == 2, beside, exp)))


def lane_of(shape):
    return lax.broadcasted_iota(jnp.int32, shape, 1)


def row_of(shape):
    return lax.broadcasted_iota(jnp.int32, shape, 0)


def bucket_of(offset):
    distance = jnp.abs(offset)
    bucket = jnp.where(offset > 0, 16, 0)
    for threshold in thresholds:
        bucket = bucket + jnp.where(distance >= threshold, 1, 0)
    return bucket


def bits_of(count):
    return count.bit_length() - 1


def column_parts(width):
    tiles = width // 128
    cuts = [0, (tiles + 2) // 3, (2 * tiles + 2) // 3, tiles]
    return [(cuts[i] * 128, (cuts[i + 1] - cuts[i]) * 128) for i in range(3)]


def flipped(place, bit):
    return place + (1 - 2 * ((place // (1 << bit)) % 2)) * (1 << bit)


class Doubling:
    def __init__(self, at, own, every, sems, core_sems, orders):
        self.at, self.own, self.every = at, own, every
        self.sems, self.core_sems, self.orders = sems, core_sems, orders
        self.plane = at.quad * at.exps + at.exp
        self.steps = len(orders[0])
        self.parts = column_parts(own.shape[1])

    def device(self, bit):
        other = flipped(self.plane, bit)
        return (self.at.grp, other // self.at.exps, other % self.at.exps)

    def place(self, part, j):
        p = self.plane
        for i, bit in enumerate(self.orders[part]):
            if (j >> i) & 1:
                p = flipped(p, bit + 1)
        return p

    def block(self, part, p):
        begin, size = self.parts[part]
        return self.every.at[p, :, pl.ds(begin, size)]

    def source(self, part, j):
        begin, size = self.parts[part]
        return self.own.at[:, pl.ds(begin, size)] if j == 0 else self.block(part, self.place(part, j))

    def index(self, step, part, j):
        return part * (1 << self.steps) + (1 << step) - 1 + j

    def copy(self, step, part, j):
        i = self.index(step, part, j)
        return send(
            self.source(part, j),
            self.block(part, self.place(part, j)),
            self.sems.at[0, i],
            self.sems.at[1, i],
            self.device(self.orders[part][step] + 1),
        )

    def core_copy(self, part, j):
        i = part * (1 << self.steps) + j
        return send(
            self.source(part, j),
            self.block(part, self.place(part, j)),
            self.core_sems.at[0, i],
            self.core_sems.at[1, i],
            self.device(0),
        )

    def start(self):
        for part in range(3):
            for step in range(self.steps):
                self.copy(step, part, 0).start()
        for part in range(3):
            self.core_copy(part, 0).start()
        self.keep().start()

    def keep(self):
        return pltpu.make_async_copy(self.own, self.every.at[self.plane], self.core_sems.at[1, 3 << self.steps])

    def next(self, step):
        for part in range(3):
            for j in range(1 << step):
                k = (1 << step) + j
                arrived(self.block(part, self.place(part, k)), self.sems.at[1, self.index(step, part, j)])
                for later in range(step + 1, self.steps):
                    self.copy(later, part, k).start()
                self.core_copy(part, k).start()

    def finish_in(self):
        for part in range(3):
            for j in range(1 << self.steps):
                there = self.block(part, flipped(self.place(part, j), 0))
                arrived(there, self.core_sems.at[1, part * (1 << self.steps) + j])
        self.keep().wait()

    def finish_out(self):
        for part in range(3):
            for j in range(1 << self.steps):
                self.core_copy(part, j).wait_send()
            for step in range(self.steps):
                for j in range(1 << step):
                    self.copy(step, part, j).wait_send()


class Halving:
    def __init__(self, at, bufs, sems, orders):
        self.at, self.bufs, self.sems = at, bufs, sems
        self.plane = at.quad * at.exps + at.exp
        self.places = bits_of(QUAD * at.exps)
        self.chip_bits = list(range(self.places - 1))
        self.parts = column_parts(bufs[0].shape[2])
        self.orders = orders

    def device(self, bit):
        other = flipped(self.plane, bit)
        return (self.at.grp, other // self.at.exps, other % self.at.exps)

    def hop(self, step, part):
        order = self.orders[part]
        bit = order[step]
        left = [b for b in self.chip_bits if b not in order[:step]]
        pos = left.index(bit)
        half = 1 << (len(left) - 1)
        mine = (self.plane // (1 << (bit + 1))) % 2
        device = self.device(bit + 1)
        begin, size = self.parts[part]
        cols = pl.ds(begin, size)
        base = self.base(step, part)

        def index(j, value):
            return (j >> pos) * (1 << (pos + 1)) + value * (1 << pos) + j % (1 << pos)

        pairs = []
        for j in range(half):
            copy = functools.partial(
                send,
                self.bufs[step].at[index(j, 1 - mine), :, cols],
                self.bufs[step + 1].at[j, :, cols],
                self.sems.at[0, base + j],
                self.sems.at[1, base + j],
                device,
            )
            pairs.append((copy, index(j, mine), j))
        return pairs, begin, size, base

    def base(self, step, part):
        n = len(self.chip_bits)
        return part * (1 << n) + sum(1 << (n - 1 - s) for s in range(step))

    def start(self, step, part=None):
        for p in range(3) if part is None else [part]:
            for copy, _, _ in self.hop(step, p)[0]:
                copy().start()

    def add(self, step, part):
        pairs, begin, size, base = self.hop(step, part)
        cols = pl.ds(begin, size)
        here, there = self.bufs[step], self.bufs[step + 1]
        for _, keep, j in pairs:
            arrived(there.at[j, :, cols], self.sems.at[1, base + j])
            there[j, :, begin : begin + size] = (
                there[j, :, begin : begin + size] + here[keep, :, begin : begin + size]
            )

    def next(self, step):
        for p in range(3):
            self.add(step, p)
            if step + 1 < len(self.chip_bits):
                self.start(step + 1, p)

    def result(self):
        return self.bufs[len(self.chip_bits)]

    def finish(self):
        for step in range(len(self.chip_bits)):
            for p in range(3):
                for copy, _, _ in self.hop(step, p)[0]:
                    copy().wait_send()


class Group:
    def __init__(self, at, own, every, sems):
        self.at, self.own, self.every, self.sems = at, own, every, sems
        self.beside, self.across = at.exp + 1 - 2 * (at.exp % 2), (at.exp + 2) % 4

    def copy(self, src, index, send_index, device):
        return send(
            src, self.every.at[index], self.sems.at[0, send_index], self.sems.at[1, index], self.at.device(self.at.rep, device)
        )

    def first(self):
        return [
            self.copy(self.own, self.at.exp, 0, self.across),
            self.copy(self.own, self.at.exp, 1, self.beside),
        ]

    def second(self):
        return self.copy(self.every.at[self.across], self.across, 2, self.beside)

    def start(self):
        for copy in self.first():
            copy.start()

    def pass_on(self):
        arrived(self.every.at[self.across], self.sems.at[1, self.across])
        self.second().start()

    def arrive(self):
        for index in (self.beside, (self.beside + 2) % 4):
            arrived(self.every.at[index], self.sems.at[1, index])

    def sent(self):
        for copy in self.first() + [self.second()]:
            copy.wait_send()


class Tiles:
    def __init__(self, units, reps):
        self.units = units
        self.reps = reps
        self.hidden = units * reps
        self.half = self.hidden // 256
        self.wide = (self.half + 1) // 2
        self.count = 3
        self.size = 128 * self.wide // self.count
        self.skip = 128 * (2 * self.wide - self.half)

    def start(self, quad):
        return 128 * (self.half * (quad // 2) + (self.half - self.wide) * (quad % 2))

    def rows(self, tile):
        result = []
        for k in range(QUAD):
            found = None
            for parity in range(2):
                first = self.start(parity) + tile * self.size
                live = first + (self.skip if parity and tile == 0 else 0)
                begin = max(live, k * self.units)
                end = min(first + self.size, (k + 1) * self.units)
                if end > begin:
                    found = (begin - k * self.units, end - begin, parity, begin - first)
            result.append(found)
        return result


class Outward:
    def __init__(self, at, tiles, tile, in_low, down_slab, both_w, down_w, nothing, sems, down_sems):
        self.at, self.tiles, self.tile = at, tiles, tile
        self.in_low, self.down_slab, self.both_w, self.down_w = in_low, down_slab, both_w, down_w
        self.nothing, self.sems, self.down_sems = nothing, sems, down_sems
        self.slab = in_low.shape[0]

    def source(self, quad, section):
        begin = section * self.tiles.hidden + self.tiles.start(quad) + self.tile * self.tiles.size
        return self.in_low.at[:, pl.ds(pl.multiple_of(begin, 128), self.tiles.size)]

    def target(self, rep, section):
        rows = pl.ds(pl.multiple_of(rep * self.slab, self.slab), self.slab)
        return self.both_w.at[rows, pl.ds(section * self.tiles.size, self.tiles.size)]

    def over(self, act):
        at = self.at

        def one(k, _):
            other = (at.rep + k) % at.reps
            for section in range(2):
                act(
                    functools.partial(
                        send,
                        self.source(other % QUAD, section),
                        self.target(at.rep, section),
                        self.sems.at[0, section * at.reps + other],
                        self.sems.at[1, section * at.reps + at.rep],
                        at.device(other, at.exp),
                    )
                )
            return 0

        lax.fori_loop(1, at.reps, one, 0)

    def over_down(self, act, act_local):
        at = self.at
        for k, piece in enumerate(self.tiles.rows(self.tile)):
            if piece is None:
                continue
            begin, count, parity, to = piece
            quad = 2 * (at.rep // QUAD) + parity
            src, dst = self.down_slab.at[pl.ds(begin, count)], self.down_w.at[pl.ds(to, count)]
            recv = self.down_sems.at[1, at.rep]
            for g in range(at.grps):
                stays = jnp.logical_and(at.grp == g, at.quad == quad)
                ours = at.rep % QUAD == k

                @pl.when(jnp.logical_and(ours, jnp.logical_not(stays)))
                def _():
                    act(functools.partial(send, src, dst, self.down_sems.at[0, g], recv, (g, quad, at.exp)))

                @pl.when(jnp.logical_and(ours, stays))
                def _():
                    act_local(functools.partial(pltpu.make_async_copy, src, dst, recv))

    def blank(self):
        return pltpu.make_async_copy(
            self.nothing, self.down_w.at[pl.ds(0, self.tiles.skip)], self.down_sems.at[1, self.at.reps]
        )

    def start(self):
        at = self.at
        self.over_down(lambda copy: copy().start(), lambda copy: copy().start())
        self.over(lambda copy: copy().start())
        for section in range(2):
            pltpu.make_async_copy(
                self.source(at.quad, section), self.target(at.rep, section), self.sems.at[1, section * at.reps + at.rep]
            ).start()
        if self.tile == 0:

            @pl.when(at.quad % 2 == 1)
            def _():
                self.blank().start()

    def arrive(self):
        at = self.at

        def one(rep, _):
            for section in range(2):
                arrived(self.target(rep, section), self.sems.at[1, section * at.reps + rep])
            return 0

        lax.fori_loop(0, at.reps, one, 0)
        for parity in range(2):

            @pl.when(at.quad % 2 == parity)
            def _():
                for k, piece in enumerate(self.tiles.rows(self.tile)):
                    if piece is not None and piece[2] == parity:
                        source = QUAD * (at.quad // 2) + k
                        arrived(self.down_w.at[pl.ds(piece[3], piece[1])], self.down_sems.at[1, source])
                if parity and self.tile == 0:
                    self.blank().wait()

    def sent(self):
        self.over(lambda copy: copy().wait_send())
        self.over_down(lambda copy: copy().wait_send(), lambda copy: None)


class Homeward:
    def __init__(self, at, tiles, tile, both, down, in_parts, down_parts, sems, down_sems, sections=(0, 1)):
        self.at, self.tiles, self.tile, self.sections = at, tiles, tile, sections
        self.both, self.down, self.in_parts, self.down_parts = both, down, in_parts, down_parts
        self.sems, self.down_sems = sems, down_sems
        self.slab = in_parts.shape[1]

    def target(self, grp, quad, parity, section):
        skip = self.tiles.skip if parity and self.tile == 0 else 0
        to = section * self.tiles.hidden + self.tiles.start(quad) + self.tile * self.tiles.size + skip
        to = to if isinstance(to, int) else pl.multiple_of(to, 128)
        return skip, self.in_parts.at[grp, :, pl.ds(to, self.tiles.size - skip)]

    def copy(self, rep, parity, section, local=False):
        at = self.at
        skip, dst = self.target(at.grp, at.quad, parity, section)
        rows = pl.ds(pl.multiple_of(rep * self.slab, self.slab), self.slab)
        src = self.both.at[rows, pl.ds(section * self.tiles.size + skip, self.tiles.size - skip)]
        recv = self.sems.at[1, section * at.reps + at.rep]
        if local:
            return pltpu.make_async_copy(src, dst, recv)
        return send(src, dst, self.sems.at[0, section * at.reps + rep], recv, at.device(rep, at.exp))

    def over(self, act, act_local):
        at = self.at
        for parity in range(2):

            @pl.when(at.quad % 2 == parity)
            def _():
                def one(k, _):
                    for section in self.sections:
                        act(self.copy((at.rep + k) % at.reps, parity, section))
                    return 0

                lax.fori_loop(1, at.reps, one, 0)
                if act_local:
                    for section in self.sections:
                        act_local(self.copy(at.rep, parity, section, local=True))

    def over_down(self, act, act_local):
        at = self.at
        if self.down is None:
            return
        for k, piece in enumerate(self.tiles.rows(self.tile)):
            if piece is None:
                continue
            begin, count, parity, to = piece
            src, dst = self.down.at[pl.ds(to, count)], self.down_parts.at[at.grp, pl.ds(begin, count)]
            recv = self.down_sems.at[1, at.grp]
            stays = jnp.logical_and(at.grp == at.quad // 2, at.quad == k)
            ours = at.quad % 2 == parity

            @pl.when(jnp.logical_and(ours, jnp.logical_not(stays)))
            def _():
                act(functools.partial(send, src, dst, self.down_sems.at[0, k], recv, (at.quad // 2, k, at.exp)))

            @pl.when(jnp.logical_and(ours, stays))
            def _():
                act_local(functools.partial(pltpu.make_async_copy, src, dst, recv))

    def start(self):
        self.over_down(lambda copy: copy().start(), lambda copy: copy().start())
        self.over(lambda copy: copy.start(), lambda copy: copy.start())

    def arrive(self):
        at = self.at
        for rep in range(at.reps):
            for section in self.sections:
                _, dst = self.target(rep // QUAD, rep % QUAD, rep % 2, section)
                arrived(dst, self.sems.at[1, section * at.reps + rep])
        for k, piece in enumerate(self.tiles.rows(self.tile)):
            if piece is None or self.down is None:
                continue

            @pl.when(at.quad == k)
            def _():
                for g in range(at.grps):
                    arrived(self.down_parts.at[g, pl.ds(piece[0], piece[1])], self.down_sems.at[1, g])

    def sent(self):
        self.over(lambda copy: copy.wait_send(), None)
        self.over_down(lambda copy: copy().wait_send(), lambda copy: None)


def forward_kernel(
    grps,
    exps,
    lengths,
    bias_table,
    routes_t,
    tokens,
    cotangent,
    gains,
    router,
    attn_qkv,
    attn_out,
    expert_in,
    expert_out,
    both_w,
    down_w,
    cot_all,
    n_all,
    comb_all,
    qkv_out,
    pb_out,
    mine_out,
    n1_out,
    wqkv_out,
    wout_out,
    h1_out,
    n2_out,
    probs_out,
    in_out,
    down_out,
    in_wide,
    down_wide,
    qkv_t,
    out_w,
    in_low,
    down_slab,
    tok_all,
    wqkv,
    wout,
    n1,
    qkv,
    pb,
    mine,
    ctx,
    bias,
    comb_send,
    nothing,
    tok_sem,
    wq_sem,
    wo_sem,
    wo2_sem,
    weight_sem,
    down_sem,
    ctx_sem,
    cot_sem,
    cot_core_sem,
    n_sem,
    n_core_sem,
    comb_sem,
    store_sem,
    cast_sem,
):
    at = Where(grps, exps)
    reps = at.reps
    rows, width = tokens.shape
    heads = HEADS // exps
    head_dim = width // HEADS
    head_cols = heads * head_dim
    block_cols = min(128, head_cols)
    shard_cols, row_block = qkv_t.shape
    seg = math.gcd(shard_cols, head_cols)
    segs = shard_cols // seg
    tiles = Tiles(down_slab.shape[0], reps)
    plane = at.quad * exps + at.exp
    members = QUAD * exps
    scale = 1.0 / math.sqrt(head_dim)
    SEND, RECV = 0, 1

    met = greet(*everyone(at))
    wide_copies = [
        pltpu.make_async_copy(expert_in, in_wide, cast_sem.at[0]),
        pltpu.make_async_copy(expert_out, down_wide, cast_sem.at[1]),
    ]
    for copy in wide_copies:
        copy.start()
    qkv_t[...] = attn_qkv[...].T.astype(low)
    out_w[...] = attn_out[...].astype(low)
    met()

    def exp_peer(k):
        return (at.exp + k) % exps

    group_tokens = Group(at, tokens, tok_all, tok_sem)
    group_tokens.start()
    tok_all[at.exp] = tokens[...]

    def segment(k):
        col = (at.rep * segs + k) * seg
        section = col // width
        within = col - section * width
        owner = within // head_cols
        return owner, section * head_cols + within - owner * head_cols

    def segment_copy(k, shift):
        owner, offset = segment(k)
        src = qkv_t.at[pl.ds(k * seg, seg)]
        dst = wqkv.at[at.exp, pl.ds(pl.multiple_of(offset, seg), seg)]
        target = at.device((at.rep + shift) % reps, owner)
        return owner, src, dst, functools.partial(
            send, src, dst, wq_sem.at[SEND, k * reps + shift], wq_sem.at[RECV, at.exp * 3 * (head_cols // seg) + offset // seg], target
        )

    def over_segments(act, act_local):
        def one(i, _):
            k, shift = i // reps, i % reps
            owner, src, dst, copy = segment_copy(k, shift)
            stays = jnp.logical_and(shift == 0, owner == at.exp)

            @pl.when(jnp.logical_not(stays))
            def _():
                act(copy())

            @pl.when(stays)
            def _():
                act_local(k, src, dst)

            return 0

        lax.fori_loop(0, segs * reps, one, 0)

    def local_segment(k, src, dst):
        _, offset = segment(k)
        pltpu.make_async_copy(src, dst, wq_sem.at[RECV, at.exp * 3 * (head_cols // seg) + offset // seg]).start()

    over_segments(lambda copy: copy.start(), local_segment)

    counterpart = (at.rep + QUAD) % reps

    def mate(k):
        return at.grp * QUAD + (at.quad + k) % QUAD

    def wout_first():
        others = [mate(k) for k in range(1, QUAD)] + [counterpart]
        return [
            send(
                out_w, wout.at[at.exp, at.rep], wo_sem.at[SEND, i], wo_sem.at[RECV, at.rep], at.device(other, at.exp)
            )
            for i, other in enumerate(others)
        ]

    def wout_passed():
        block = wout.at[at.exp, counterpart]
        return [
            send(block, block, wo_sem.at[SEND, QUAD + k - 1], wo_sem.at[RECV, counterpart], at.device(mate(k), at.exp))
            for k in range(1, QUAD)
        ]

    for copy in wout_first():
        copy.start()
    wout[at.exp, at.rep] = out_w[...]
    chip_bits = list(range(bits_of(members) - 1))
    cots = Doubling(at, cotangent, cot_all, cot_sem, cot_core_sem, [chip_bits[::-1]] * 3)
    cots.start()

    span = 2 * rows
    bucket = bucket_of(lane_of((8, span)) - rows)
    for h in range(heads):
        line = jnp.zeros((8, span), full)
        for b in range(BUCKETS):
            line = jnp.where(bucket == b, bias_table[at.exp * heads + h, b], line)
        whole = jnp.broadcast_to(line[0:1], (rows, span))
        bias[h] = pltpu.roll(whole, 0, 1, stride=1, stride_axis=0)[:, rows:]

    group_tokens.pass_on()
    group_tokens.arrive()

    def norm_group(s, _):
        x = tok_all[s].astype(full)
        r = lax.rsqrt(jnp.mean(x * x, axis=1, keepdims=True) + eps_norm)
        n1[s] = (x * r * gains[0:1, :]).astype(low)
        return 0

    lax.fori_loop(0, exps, norm_group, 0)

    for copy in wide_copies:
        copy.wait()
    in_low[...] = in_wide[...].astype(low)
    down_slab[...] = down_wide[...].astype(low)
    nothing[...] = jnp.zeros_like(nothing)
    weights = [
        Outward(
            at, tiles, t, in_low, down_slab, both_w.at[t], down_w.at[t], nothing, weight_sem.at[t], down_sem.at[t]
        )
        for t in range(2)
    ]

    weights[0].start()

    def wait_segment(i, _):
        e, j = i // (3 * head_cols // seg), i % (3 * head_cols // seg)
        arrived(wqkv.at[e, pl.ds(pl.multiple_of(j * seg, seg), seg)], wq_sem.at[RECV, i])
        return 0

    lax.fori_loop(0, exps * 3 * head_cols // seg, wait_segment, 0)

    def project(s, _):
        total = jnp.zeros((rows, 3 * head_cols), full)
        for e in range(exps):
            total = total + nt(n1[s, :, e * row_block : (e + 1) * row_block], wqkv[e])
        qkv[s] = total.astype(low)
        return 0

    lax.fori_loop(0, exps, project, 0)

    group_wout = Group(at, wout.at[at.exp], wout, wo2_sem)

    def beside(k):
        if k == 1:
            arrived(wout.at[at.exp, counterpart], wo_sem.at[RECV, counterpart])
            for copy in wout_passed():
                copy.start()
        elif k == 2:
            for j in range(1, QUAD):
                for other in (mate(j), (mate(j) + QUAD) % reps):
                    arrived(wout.at[at.exp, other], wo_sem.at[RECV, other])
            group_wout.start()
            cots.next(0)
        else:
            group_wout.pass_on()

    def attend(i, _):
        s = turn(at.exp, i)
        for k in range(1, exps):

            @pl.when(i == k)
            def _():
                beside(k)

        ok = lane_of((rows, rows)) < lengths[at.base + s]
        lane = lane_of((rows, block_cols))
        for c in range(head_cols // block_cols):
            cols = slice(c * block_cols, (c + 1) * block_cols)
            q = qkv[s, :, cols] * scale
            k = qkv[s, :, head_cols + c * block_cols : head_cols + (c + 1) * block_cols]
            v = qkv[s, :, 2 * head_cols + c * block_cols : 2 * head_cols + (c + 1) * block_cols]
            result = jnp.zeros((rows, block_cols), full)
            for t in range(block_cols // head_dim):
                h = c * (block_cols // head_dim) + t
                here = jnp.logical_and(lane >= t * head_dim, lane < (t + 1) * head_dim)
                scores = nt(jnp.where(here, q, jnp.zeros_like(q)), k) + bias[h]
                scores = jnp.where(ok, scores, -1e30)
                top = jnp.max(scores, axis=1, keepdims=True)
                weights = jnp.exp(scores - top)
                total = jnp.sum(weights, axis=1, keepdims=True)
                weights = (weights * (1.0 / total)).astype(low)
                result = jnp.where(here, jnp.dot(weights, v, preferred_element_type=full), result)
                pb[s * heads + h] = weights
            mine[s, :, cols] = result.astype(low)

        @pl.when(i < exps - 1)
        def _():
            send(
                mine.at[s], ctx.at[at.exp], ctx_sem.at[SEND, s], ctx_sem.at[RECV, at.exp], at.device(at.rep, s)
            ).start()

        @pl.when(i == exps - 1)
        def _():
            pltpu.make_async_copy(mine.at[s], ctx.at[at.exp], ctx_sem.at[RECV, at.exp]).start()

        return 0

    lax.fori_loop(0, exps, attend, 0)

    cots.next(1)
    group_wout.arrive()
    for e in range(exps):
        arrived(ctx.at[e], ctx_sem.at[RECV, e])

    out_cols = wout.shape[3]
    for r in range(reps):
        cols = slice(r * out_cols, (r + 1) * out_cols)
        total = tokens[:, cols].astype(full)
        for e in range(exps):
            total = total + jnp.dot(ctx[e], wout[e, r], preferred_element_type=full)
        h1_out[:, cols] = total
    h1 = h1_out[...]
    r2 = lax.rsqrt(jnp.mean(h1 * h1, axis=1, keepdims=True) + eps_norm)
    n2 = (h1 * r2 * gains[1:2, :]).astype(low)
    n2_out[...] = n2
    rotated = [chip_bits[c:] + chip_bits[:c] for c in range(3)]
    rows_two = Doubling(at, n2_out, n_all, n_sem, n_core_sem, rotated)
    rows_two.start()
    weights[1].start()

    router_rows = jnp.concatenate([router[...], jnp.zeros((128 - exps, width), full)], axis=0)
    logits = nt(n2.astype(full), router_rows, precision=highest)
    lane = lane_of((rows, 128))
    logits = jnp.where(lane < exps, logits, -1e30)
    probs = jnp.exp(logits - jnp.max(logits, axis=1, keepdims=True))
    probs = probs / jnp.sum(probs, axis=1, keepdims=True)
    probs_out[...] = probs
    picked = jnp.where(routed(routes_t, at.me, rows), probs, 0.0)
    comb = picked / jnp.sum(picked, axis=1, keepdims=True)
    comb = jnp.where(row_of((rows, 1)) < lengths[at.me], comb, 0.0)
    comb_send[...] = comb.T[0 : comb_send.shape[0]]

    def comb_copy(k):
        other = (plane + k) % members
        return send(
            comb_send,
            comb_all.at[plane],
            comb_sem.at[SEND, other],
            comb_sem.at[RECV, plane],
            (at.grp, other // exps, other % exps),
        )

    def start_comb(k, _):
        comb_copy(k).start()
        return 0

    lax.fori_loop(1, members, start_comb, 0)
    pltpu.make_async_copy(comb_send, comb_all.at[plane], comb_sem.at[RECV, plane]).start()
    rows_two.next(0)

    stores = [
        (qkv, qkv_out),
        (pb, pb_out),
        (mine, mine_out),
        (n1, n1_out),
        (wqkv, wqkv_out),
        (wout, wout_out),
        (in_low, in_out),
        (down_slab, down_out),
    ]
    for i, (src, dst) in enumerate(stores):
        pltpu.make_async_copy(src, dst, store_sem.at[i]).start()

    for step in range(1, rows_two.steps):
        rows_two.next(step)
    for step in range(2, cots.steps):
        cots.next(step)

    cots.finish_in()
    rows_two.finish_in()

    def comb_in(k, _):
        arrived(comb_all.at[k], comb_sem.at[RECV, k])
        return 0

    lax.fori_loop(0, members, comb_in, 0)
    for tile in weights:
        tile.arrive()

    for k in range(1, exps):
        peer = exp_peer(k)
        arrived(mine.at[peer], ctx_sem.at[SEND, peer])
    over_segments(lambda copy: copy.wait_send(), lambda k, src, dst: None)
    for copy in wout_first() + wout_passed():
        copy.wait_send()
    group_tokens.sent()
    group_wout.sent()
    cots.finish_out()
    rows_two.finish_out()

    def sent_comb(k, _):
        comb_copy(k).wait_send()
        return 0

    lax.fori_loop(1, members, sent_comb, 0)
    for tile in weights:
        tile.sent()
    for i, (src, dst) in enumerate(stores):
        pltpu.make_async_copy(src, dst, store_sem.at[i]).wait()


def forward_call(
    grps, exps, lengths, bias_table, routes_t, tokens, cotangent, gains, router, attn_qkv, attn_out, expert_in, expert_out
):
    reps = grps * QUAD
    rows, width = tokens.shape
    head_cols = width // exps
    row_block, shard_cols = attn_qkv.shape
    seg = math.gcd(shard_cols, head_cols)
    segs = shard_cols // seg
    units = expert_out.shape[0]
    out_cols = attn_out.shape[1]
    heads = HEADS // exps
    members = QUAD * exps
    tiles = Tiles(units, reps)
    shape = jax.ShapeDtypeStruct
    vmem = pl.BlockSpec(memory_space=pltpu.VMEM)
    smem = pl.BlockSpec(memory_space=pltpu.SMEM)
    hbm = pl.BlockSpec(memory_space=pl.ANY)
    results = [
        (shape((2, width, 2 * tiles.size), low), hbm),
        (shape((2, tiles.size, width), low), hbm),
        (shape((members, rows, width), low), hbm),
        (shape((members, rows, width), low), hbm),
        (shape((members, 8, rows), full), hbm),
        (shape((exps, rows, 3 * head_cols), low), hbm),
        (shape((exps * heads, rows, rows), low), hbm),
        (shape((exps, rows, head_cols), low), hbm),
        (shape((exps, rows, width), low), hbm),
        (shape((exps, 3 * head_cols, row_block), low), hbm),
        (shape((exps, reps, row_block, out_cols), low), hbm),
        (shape((rows, width), full), vmem),
        (shape((rows, width), low), vmem),
        (shape((rows, 128), full), vmem),
        (shape(expert_in.shape, low), hbm),
        (shape(expert_out.shape, low), hbm),
    ]
    dma = pltpu.SemaphoreType.DMA
    chips = members // 2
    return pl.pallas_call(
        functools.partial(forward_kernel, grps, exps),
        out_shape=[r[0] for r in results],
        in_specs=[smem] * 2 + [vmem] * 7 + [hbm] * 2,
        out_specs=[r[1] for r in results],
        scratch_shapes=[
            pltpu.VMEM(expert_in.shape, full),
            pltpu.VMEM(expert_out.shape, full),
            pltpu.VMEM((shard_cols, row_block), low),
            pltpu.VMEM((row_block, out_cols), low),
            pltpu.VMEM(expert_in.shape, low),
            pltpu.VMEM(expert_out.shape, low),
            pltpu.VMEM((exps, rows, width), low),
            pltpu.VMEM((exps, 3 * head_cols, row_block), low),
            pltpu.VMEM((exps, reps, row_block, out_cols), low),
            pltpu.VMEM((exps, rows, width), low),
            pltpu.VMEM((exps, rows, 3 * head_cols), low),
            pltpu.VMEM((exps * heads, rows, rows), low),
            pltpu.VMEM((exps, rows, head_cols), low),
            pltpu.VMEM((exps, rows, head_cols), low),
            pltpu.VMEM((heads, rows, rows), full),
            pltpu.VMEM((8, rows), full),
            pltpu.VMEM((tiles.skip, width), low),
            dma((2, exps)),
            dma((2, max(segs * reps, exps * 3 * head_cols // seg))),
            dma((2, reps)),
            dma((2, exps)),
            dma((2, 2, 2 * reps)),
            dma((2, 2, reps + 1)),
            dma((2, exps)),
            dma((2, 3 * chips)),
            dma((2, 3 * chips + 1)),
            dma((2, 3 * chips)),
            dma((2, 3 * chips + 1)),
            dma((2, members)),
            dma((8,)),
            dma((2,)),
        ],
        compiler_params=pltpu.CompilerParams(
            collective_id=0, has_side_effects=True, vmem_limit_bytes=60 * 1024 * 1024
        ),
        name="forward",
    )(lengths, bias_table, routes_t, tokens, cotangent, gains, router, attn_qkv, attn_out, expert_in, expert_out)


def expert_kernel(
    grps,
    exps,
    cap,
    deal,
    routes_t,
    comb,
    n_all,
    cot_all,
    both_w,
    down_w,
    in_low,
    down_slab,
    h1,
    n_total,
    y_half,
    y_far,
    c_in,
    both_g,
    down_g,
    in_parts,
    down_parts,
    place,
    marks,
    n_rows,
    g_rows,
    both_v,
    down_v,
    raw_n,
    raw_g,
    y_acc,
    n_acc,
    both_d,
    active,
    n_bufs,
    c_sum,
    out_y,
    load_sem,
    raw_sem,
    out_sem,
    in_sem,
    in_down_sem,
    home_sem,
    home_down_sem,
    stage_sem,
    far_sem,
    n_sem,
    c_sem,
):
    at = Where(grps, exps)
    rows, width = n_all.shape[1:]
    tiles = Tiles(down_slab.shape[0], at.reps)
    size = tiles.size
    slots = exps * cap
    members = QUAD * exps
    loads = [pltpu.make_async_copy(both_w.at[t], both_v.at[t], load_sem.at[0, t]) for t in range(2)] + [
        pltpu.make_async_copy(down_w.at[t], down_v.at[t], load_sem.at[1, t]) for t in range(2)
    ]
    for copy in loads:
        copy.start()

    def raw_copies(q):
        here = pl.ds(pl.multiple_of(q * exps, exps), exps)
        return [
            pltpu.make_async_copy(n_all.at[here], raw_n.at[pl.ds(q % 2 * exps, exps)], raw_sem.at[0, q % 2]),
            pltpu.make_async_copy(cot_all.at[here], raw_g.at[pl.ds(q % 2 * exps, exps)], raw_sem.at[1, q % 2]),
        ]

    for copy in raw_copies(0):
        copy.start()

    beside = at.exp + 1 - 2 * (at.exp % 2)
    greet(*neighbours(at))()
    last = tiles.count - 1
    incoming = Outward(
        at, tiles, last, in_low, down_slab, both_v.at[last], down_v.at[last], None, in_sem, in_down_sem
    )
    incoming.start()
    home = Homeward(
        at, tiles, 0, both_v.at[0], down_v.at[0], in_parts, down_parts, home_sem, home_down_sem
    )

    earlier = jnp.where(row_of((rows, rows)) < lane_of((rows, rows)), 1.0, 0.0).astype(low)
    slot = row_of((cap, rows)).astype(full)

    def dispatch(q, _):
        @pl.when(q + 1 < QUAD)
        def _():
            for copy in raw_copies(q + 1):
                copy.start()

        for copy in raw_copies(q):
            copy.wait()
        lines = []
        for j in range(exps):
            seq = at.grp * members + q * exps + j
            pair = routes_t[:, pl.ds(pl.multiple_of(seq * rows, rows), rows)]
            lines.append(jnp.logical_or(pair[0:1] == at.exp, pair[1:2] == at.exp))
        lines = [jnp.where(line, 1.0, 0.0) for line in lines] + [jnp.zeros((8 - exps, rows), full)]
        hot_low = jnp.concatenate(lines, axis=0).astype(low)
        before = dot(hot_low, earlier)
        for j in range(exps):
            s = q * exps + j
            inside = jnp.logical_and(slot == before[j : j + 1, :], hot_low[j : j + 1, :].astype(full) > 0.5)
            here = jnp.where(inside, 1.0, 0.0)
            place[s] = here.astype(low)
            g = raw_g[q % 2 * exps]
            for b in range(1, exps):
                g = jnp.where(deal[at.grp * members + s] == at.grp * members + q * exps + b, raw_g[q % 2 * exps + b], g)
            where = pl.ds(pl.multiple_of(s * cap, cap), cap)
            n_rows[where] = dot(here.astype(low), raw_n[q % 2 * exps + j]).astype(low)
            g_rows[where] = dot(here.astype(low), g).astype(low)
            marks[where, 0:1] = jnp.sum(here * comb[s, pl.ds(at.exp, 1), :], axis=1, keepdims=True)
            marks[where, 1:2] = jnp.zeros((cap, 1), full)
        return 0

    lax.fori_loop(0, QUAD, dispatch, 0)
    for copy in loads:
        copy.wait()
    curve = math.sqrt(2.0 / math.pi)

    core = at.exp % 2

    plane = at.quad * exps + at.exp
    sibling = at.device(at.rep, beside)
    dn = Halving(at, n_bufs, n_sem, [[0, 1, 2], [1, 2, 0], [2, 0, 1]])

    def n_copy(j):
        return send(raw_n.at[j], n_bufs[0].at[j], far_sem.at[0, 0, j], far_sem.at[0, 1, j], sibling)

    def y_copies(j):
        return (
            pltpu.make_async_copy(out_y.at[j % 2], y_half.at[j], out_sem.at[j % 2]),
            send(raw_n.at[j], y_far.at[j], far_sem.at[1, 0, j], far_sem.at[1, 1, j], sibling),
        )

    def c_copy(k):
        other = (plane + k) % members
        return send(
            c_sum.at[other],
            c_in.at[plane],
            c_sem.at[0, other],
            c_sem.at[1, plane],
            (at.grp, other // exps, other % exps),
        )

    def slots_of(s):
        return pl.ds(pl.multiple_of(s * cap, cap), cap)

    def n_rows_of(s):
        where = slots_of(s)
        line = jnp.sum(place[s].astype(full) * marks[where, 1:2], axis=0, keepdims=True)
        c_sum[s] = jnp.broadcast_to(line, (8, rows))
        return tn(place[s], n_acc[where]).astype(low)

    def y_rows_of(p):
        first = p // exps * exps
        spot = at.grp * members + p
        here, y = place[first], y_acc[slots_of(first)]
        for c in range(1, exps):
            taken = deal[at.grp * members + first + c] == spot
            here = jnp.where(taken, place[first + c], here)
            y = jnp.where(taken, y_acc[slots_of(first + c)], y)
        return (tn(here, y) + jnp.where(deal[at.me] == spot, h1[...], 0.0)).astype(low)

    def give_n(j):
        raw_n[j] = n_rows_of(2 * j + 1 - core)
        n_copy(j).start()
        raw_g[j] = n_rows_of(2 * j + core)

    def add_n(quad):
        for k in range(exps // 2):
            j = quad * (exps // 2) + k
            arrived(n_bufs[0].at[j], far_sem.at[0, 1, j])
            n_bufs[0][j] = n_bufs[0][j] + raw_g[j]

    def give_y(j, _):
        @pl.when(j >= 2)
        def _():
            y_copies(j - 2)[0].wait()

        out_y[j % 2] = y_rows_of(2 * j + core)
        n_copy(j).wait_send()
        raw_n[j] = y_rows_of(2 * j + 1 - core)
        for copy in y_copies(j):
            copy.start()
        return 0

    def start_c(k, _):
        c_copy(k).start()
        return 0

    def tile_work(f, _):
        @pl.when(f == last)
        def _():
            incoming.arrive()
            home.start()

        def chunk(i, _):
            c = jnp.where(i == 0, at.near(3), jnp.where(i == 1, at.near(1), jnp.where(i == 2, at.near(2), at.quad)))
            here = pl.ds(pl.multiple_of(c * slots, slots), slots)
            share = marks[here, 0:1]
            both = dot(n_rows[here], both_v[f])
            gate_part, up_part = both[:, :size], both[:, size:]
            grad = nt(g_rows[here], down_v[f])
            square = gate_part * gate_part
            bend = jnp.tanh(curve * gate_part * (1.0 + 0.044715 * square))
            half = 0.5 * (1.0 + bend)
            gelu = gate_part * half
            slope = half + (0.5 * curve) * gate_part * (1.0 - bend * bend) * (1.0 + (3 * 0.044715) * square)
            value = gelu * up_part
            marks[here, 1:2] += jnp.sum(value * grad, axis=1, keepdims=True)
            grad = grad * share
            active[f % 2, here] = (value * share).astype(low)
            both_d[f % 2, here, :size] = (grad * up_part * slope).astype(low)
            both_d[f % 2, here, size:] = (grad * gelu).astype(low)
            y = dot(active[f % 2, here], down_v[f])
            y_acc[here] = jnp.where(f == 0, y, y_acc[here].astype(full) + y).astype(low)
            n_back = nt(both_d[f % 2, here], both_v[f])
            n_acc[here] = jnp.where(f == 0, n_back, n_acc[here].astype(full) + n_back).astype(low)

            @pl.when(f == last)
            def _():
                for k in range(exps // 2):
                    give_n(c * (exps // 2) + k)

            @pl.when(jnp.logical_and(f == last, i == 2))
            def _():
                add_n(at.near(3))

            @pl.when(jnp.logical_and(f == last, i == 3))
            def _():
                add_n(at.near(1))
                dn.start(0, 1)

            return 0

        lax.fori_loop(0, QUAD, chunk, 0)

        @pl.when(f == 0)
        def _():
            weight_work(0)

        return 0

    def weight_work(f):
        def columns(m, _):
            cols = pl.ds(pl.multiple_of(m * (width // 2), width // 2), width // 2)
            both_v[f, cols] = tn(n_rows[:, cols], both_d[f % 2]).astype(low)
            down_v[f, :, cols] = tn(active[f % 2], g_rows[:, cols]).astype(low)
            return 0

        lax.fori_loop(0, 2, columns, 0)

        for copy in stage_copies(f):
            copy.start()

    def stage_copies(f):
        if f == 0:
            return []
        return [
            pltpu.make_async_copy(both_v.at[f], both_g.at[f - 1], stage_sem.at[0, f]),
            pltpu.make_async_copy(down_v.at[f], down_g.at[f - 1], stage_sem.at[1, f]),
        ]

    lax.fori_loop(0, tiles.count, tile_work, 0)

    half = members // 2
    lax.fori_loop(1, members, start_c, 0)
    c_in[plane] = c_sum[plane]
    weight_work(1)
    add_n(at.near(2))
    dn.start(0, 2)
    add_n(at.quad)
    dn.start(0, 0)
    weight_work(2)
    lax.fori_loop(0, half, give_y, 0)
    for step in range(len(dn.chip_bits)):
        dn.next(step)
    n_total[...] = dn.result()[0]
    for j in (half - 2, half - 1):
        y_copies(j)[0].wait()
    for f in range(tiles.count):
        for copy in stage_copies(f):
            copy.wait()

    def core_in(j, _):
        y_copies(j)[1].wait_send()
        arrived(y_far.at[j], far_sem.at[1, 1, j])
        return 0

    lax.fori_loop(0, half, core_in, 0)

    def c_done(k, _):
        c_copy(k).wait_send()
        other = (plane + k) % members
        arrived(c_in.at[other], c_sem.at[1, other])
        return 0

    lax.fori_loop(1, members, c_done, 0)
    dn.finish()
    home.arrive()
    incoming.sent()
    home.sent()


def expert_call(grps, exps, cap, deal, routes_t, comb_all, n_all, cot_all, both_w, down_w, in_low, down_slab, h1):
    members, rows, width = n_all.shape
    reps = grps * QUAD
    tiles = Tiles(down_slab.shape[0], reps)
    size = tiles.size
    slab, both_hidden = in_low.shape
    units = down_slab.shape[0]
    slots = exps * cap
    chip_bits = bits_of(members) - 1
    shape = jax.ShapeDtypeStruct
    vmem = pl.BlockSpec(memory_space=pltpu.VMEM)
    smem = pl.BlockSpec(memory_space=pltpu.SMEM)
    hbm = pl.BlockSpec(memory_space=pl.ANY)
    results = [
        (shape((rows, width), low), vmem),
        (shape((members // 2, rows, width), low), hbm),
        (shape((members // 2, rows, width), low), hbm),
        (shape((members, 8, rows), full), vmem),
        (shape((2, width, 2 * size), low), hbm),
        (shape((2, size, width), low), hbm),
        (shape((grps, slab, both_hidden), low), hbm),
        (shape((grps, units, width), low), hbm),
    ]
    dma = pltpu.SemaphoreType.DMA
    return pl.pallas_call(
        functools.partial(expert_kernel, grps, exps, cap),
        out_shape=[r[0] for r in results],
        in_specs=[smem] + [vmem] * 2 + [hbm] * 6 + [vmem],
        out_specs=[r[1] for r in results],
        scratch_shapes=[
            pltpu.VMEM((members, cap, rows), low),
            pltpu.VMEM((QUAD * slots, 128), full),
            pltpu.VMEM((QUAD * slots, width), low),
            pltpu.VMEM((QUAD * slots, width), low),
            pltpu.VMEM((tiles.count, width, 2 * size), low),
            pltpu.VMEM((tiles.count, size, width), low),
            pltpu.VMEM((2 * exps, rows, width), low),
            pltpu.VMEM((2 * exps, rows, width), low),
            pltpu.VMEM((QUAD * slots, width), low),
            pltpu.VMEM((QUAD * slots, width), low),
            pltpu.VMEM((2, QUAD * slots, 2 * size), low),
            pltpu.VMEM((2, QUAD * slots, size), low),
            [pltpu.VMEM((members >> (1 + step), rows, width), low) for step in range(chip_bits + 1)],
            pltpu.VMEM((members, 8, rows), full),
            pltpu.VMEM((2, rows, width), low),
            dma((2, 2)),
            dma((2, 2)),
            dma((2,)),
            dma((2, 2 * reps)),
            dma((2, reps + 1)),
            dma((2, 2 * reps)),
            dma((2, max(QUAD, grps))),
            dma((2, tiles.count)),
            dma((2, 2, members // 2)),
            dma((2, 3 << chip_bits)),
            dma((2, members)),
        ],
        compiler_params=pltpu.CompilerParams(
            collective_id=2, has_side_effects=True, vmem_limit_bytes=60 * 1024 * 1024
        ),
        name="experts",
    )(deal, routes_t, comb_all, n_all, cot_all, both_w, down_w, in_low, down_slab, h1)


def adamw_root(weight, moment, second, gradient, step_rate, decay_factor):
    new_moment = beta_one * moment + (1.0 - beta_one) * gradient
    new_second = beta_two * second + (1.0 - beta_two) * gradient * gradient
    root = lax.rsqrt(new_second * (1.0 / (1.0 - beta_two**STEP)))
    step = new_moment * (root * (1.0 - eps_adam * root))
    keep = 1.0 - step_rate * decay_factor
    return (new_moment, new_second, keep * weight - (step_rate / (1.0 - beta_one**STEP)) * step)


def adam_kernel(exps, *refs):
    in_parts, down_parts, qkv_grad, out_grad, small = refs[:5]
    states, news, bias_grad = refs[5:26], refs[26:47], refs[47]
    heads = HEADS // exps
    width = small.shape[1]

    def update(i, grad, rate, decay):
        weight, first, second = [state[...] for state in states[3 * i : 3 * i + 3]]
        values = adamw_root(weight, first, second, grad, rate, decay)
        for new, value in zip(news[3 * i : 3 * i + 3], values, strict=True):
            new[...] = value

    def total(parts):
        result = parts[0].astype(full)
        for k in range(1, parts.shape[0]):
            result = result + parts[k].astype(full)
        return result

    @pl.when(pl.program_id(0) == 0)
    def _():
        update(0, qkv_grad[...], 1.5 / math.sqrt(D), 0.1)
        update(1, out_grad[...], 6.0 / math.sqrt(D), 0.1)
        for e in range(exps):
            for h in range(heads):
                bias_grad[e * heads + h : e * heads + h + 1, :] = small[
                    exps + 3 + e : exps + 4 + e, h * 128 : h * 128 + BUCKETS
                ]
        update(2, bias_grad[...], 0.3, 0.0)
        update(3, small[0:exps, :], 1.0 / math.sqrt(D), 0.1)
        update(4, small[exps : exps + 2, :], 0.5, 0.0)

    update(5, total(in_parts), 1.5 / math.sqrt(D), 0.1)
    update(6, total(down_parts), 1.5 / math.sqrt(FF), 0.1)


def adam_call(exps, in_parts, down_parts, qkv_grad, out_grad, small, states):
    steps = 4

    def whole(array):
        return pl.BlockSpec(array.shape, lambda i: (0,) * array.ndim)

    def columns(array):
        block = array.shape[:-1] + (array.shape[-1] // steps,)
        return pl.BlockSpec(block, lambda i: (0,) * (array.ndim - 1) + (i,))

    specs = [whole(state) for state in states[:15]]
    specs += [columns(state) for state in states[15:18]] + [columns(state) for state in states[18:]]
    return pl.pallas_call(
        functools.partial(adam_kernel, exps),
        grid=(steps,),
        in_specs=[columns(in_parts), columns(down_parts), whole(qkv_grad), whole(out_grad), whole(small)] + specs,
        out_specs=specs,
        out_shape=[jax.ShapeDtypeStruct(state.shape, full) for state in states],
        scratch_shapes=[pltpu.VMEM((HEADS, BUCKETS), full)],
        compiler_params=pltpu.CompilerParams(vmem_limit_bytes=60 * 1024 * 1024),
        name="adam",
    )(in_parts, down_parts, qkv_grad, out_grad, small, *states)


def backward_kernel(
    grps,
    exps,
    lengths,
    deal,
    y_half,
    y_far,
    both_g,
    down_g,
    in_before,
    down_before,
    n1_in,
    cot_all,
    routes_t,
    tokens,
    n_total,
    c_in,
    n2_in,
    probs_in,
    h1_from,
    qkv_from,
    pb_from,
    mine_from,
    wqkv_from,
    wout_from,
    gains,
    router_t,
    *rest,
):
    token_grad, block_out, in_parts, down_parts, qkv_grad, out_grad, small_out = rest[:7]
    scratch = rest[7:]
    (
    h1_in,
    qkv,
    pb,
    mine,
    wqkv,
    wout,
    kept,
    y_bufs,
    dh1,
    dz_send,
    dz_all,
    do_send,
    do_in,
    bias_sum,
    dqkv,
    dqkv_t,
    dn1_send,
    dn1_in,
    wq_send,
    og_send,
    mids,
    far_send,
    far_in,
    small_send,
    small_exp,
    small_sum,
    small_rep,
    small_half,
    small_far,
    y_sem,
    load_sem,
    weight_sem,
    down_sem,
    dz_sem,
    do_sem,
    dn1_sem,
    wq_sem,
    og_sem,
    mid_sem,
    far_sem,
    small_sem,
    small2_sem,
    small3_sem,
    n1_sem,
    operand_sem,
    ) = scratch
    at = Where(grps, exps)
    reps = at.reps
    rows, width = tokens.shape
    heads = HEADS // exps
    head_dim = width // HEADS
    head_cols = heads * head_dim
    block_cols = min(128, head_cols)
    row_block = wqkv.shape[2]
    out_cols = wout.shape[3]
    tiles = Tiles(down_parts.shape[1], reps)
    scale = 1.0 / math.sqrt(head_dim)
    SEND, RECV = 0, 1
    plane = at.quad * exps + at.exp
    members = QUAD * exps

    def exp_peer(k):
        return (at.exp + k) % exps

    router = router_t[...]
    met = greet(*neighbours(at))
    n1 = kept.at[0:exps]
    group = pl.ds(pl.multiple_of(at.quad * exps, exps), exps)
    cot_copy = pltpu.make_async_copy(cot_all.at[group], dn1_send, n1_sem.at[1])
    cot_copy.start()
    loads = [
        pltpu.make_async_copy(src, dst, operand_sem.at[i])
        for i, (src, dst) in enumerate(
            ((h1_from, h1_in), (wout_from, wout), (qkv_from, qkv), (pb_from, pb), (mine_from, mine), (wqkv_from, wqkv))
        )
    ]
    ys = Halving(at, y_bufs, y_sem, [[0, 1, 2], [0, 1, 2], [1, 0, 2]])
    half_loads = [
        pltpu.make_async_copy(y_far, y_bufs[0], load_sem.at[0]),
        pltpu.make_async_copy(y_half, kept, load_sem.at[1]),
    ]
    for copy in loads + half_loads:
        copy.start()

    span = 2 * rows
    met()

    homes = [
        Homeward(
            at, tiles, t + 1, both_g.at[t], down_g.at[t], in_parts, down_parts, weight_sem.at[t], down_sem.at[t]
        )
        for t in range(2)
    ]
    homes[0].start()
    n1_copy = pltpu.make_async_copy(n1_in, n1, n1_sem.at[0])

    lane = lane_of((rows, 128))
    comb_rows = []
    for e in range(exps):
        total = c_in[e]
        for q in range(1, QUAD):
            total = total + c_in[q * exps + e]
        comb_rows.append(total[0:1, :])
    comb_rows.append(jnp.zeros((128 - exps, rows), full))
    comb_grad = jnp.concatenate(comb_rows, axis=0).T
    valid = row_of((rows, 1)) < lengths[at.me]
    probs = probs_in[...]
    hot = routed(routes_t, at.me, rows)
    picked = jnp.where(hot, probs, 0.0)
    total = jnp.sum(picked, axis=1, keepdims=True)
    gate = picked / total
    gate_grad_rows = jnp.where(valid, comb_grad, 0.0)
    spread_grad = jnp.sum(gate_grad_rows * gate, axis=1, keepdims=True)
    probs_grad = jnp.where(hot, (gate_grad_rows - spread_grad) / total, 0.0)
    logit_grad = probs * (probs_grad - jnp.sum(probs_grad * probs, axis=1, keepdims=True))
    small_rows = small_send.shape[0]
    small_send[...] = jnp.zeros_like(small_send)
    router_back = jnp.dot(
        logit_grad, jnp.concatenate([router, jnp.zeros((128 - exps, width), full)], axis=0),
        precision=highest, preferred_element_type=full,
    )
    for copy in loads:
        copy.wait()
    h1 = h1_in[...]
    r2 = lax.rsqrt(jnp.mean(h1 * h1, axis=1, keepdims=True) + eps_norm)

    steps = len(ys.chip_bits)
    n2_grad = router_back + n_total[...].astype(full)
    scaled = n2_grad * gains[1:2, :]
    cot_copy.wait()
    dealt = deal[at.me] - at.base
    g = dn1_send[0]
    for e in range(1, exps):
        g = jnp.where(dealt == e, dn1_send[e], g)
    hidden_grad = (
        jnp.where(valid, g.astype(full), 0.0)
        + r2 * scaled
        - h1 * (r2 * r2 * r2) * jnp.mean(scaled * h1, axis=1, keepdims=True)
    )
    dh1[...] = hidden_grad
    small_send[exps + 1 : exps + 2, :] = jnp.sum(n2_grad * h1 * r2, axis=0, keepdims=True)
    branch = hidden_grad.astype(low)
    dz_send[...] = branch
    for e in range(exps):
        total = jnp.zeros((rows, row_block), full)
        for r in range(reps):
            total = total + nt(branch[:, r * out_cols : (r + 1) * out_cols], wout[e, r])
        do_send[e] = total.astype(low)

    def do_copies():
        return [
            send(
                do_send.at[exp_peer(k)],
                do_in.at[at.exp],
                do_sem.at[SEND, exp_peer(k)],
                do_sem.at[RECV, at.exp],
                at.device(at.rep, exp_peer(k)),
            )
            for k in range(1, exps)
        ]

    for copy in do_copies():
        copy.start()
    pltpu.make_async_copy(do_send.at[at.exp], do_in.at[at.exp], do_sem.at[RECV, at.exp]).start()

    group_dz = Group(at, dz_send, dz_all, dz_sem)
    dz_all[at.exp] = branch
    for copy in half_loads:
        copy.wait()

    def add_halves(j, _):
        y_bufs[0][j] = y_bufs[0][j] + kept[j]
        return 0

    lax.fori_loop(0, kept.shape[0], add_halves, 0)
    n1_copy.start()

    bias_sum[...] = jnp.zeros_like(bias_sum)

    def dn1_copies():
        beside, across = turn(at.exp, 2), turn(at.exp, 1)
        return [
            functools.partial(
                send, dn1_send.at[k], dn1_in.at[j], dn1_sem.at[SEND, j], dn1_sem.at[RECV, j], at.device(at.rep, to)
            )
            for k, j, to in ((turn(at.exp, 0), 2, beside), (across, 0, across), (beside, 1, beside))
        ]

    def attend_back(i, _):
        s = turn(at.exp, i)
        arrived(do_in.at[s], do_sem.at[RECV, s])

        @pl.when(i == 0)
        def _():
            group_dz.start()
            ys.start(0)

        @pl.when(i == 1)
        def _():
            homes[1].start()

        @pl.when(i == 2)
        def _():
            group_dz.pass_on()

        block_lane = lane_of((rows, block_cols))
        for c in range(head_cols // block_cols):
            cols = slice(c * block_cols, (c + 1) * block_cols)
            k_cols = slice(head_cols + c * block_cols, head_cols + (c + 1) * block_cols)
            v_cols = slice(2 * head_cols + c * block_cols, 2 * head_cols + (c + 1) * block_cols)
            q = qkv[s, :, cols] * scale
            k = qkv[s, :, k_cols]
            v = qkv[s, :, v_cols]
            do = do_in[s, :, cols]
            dq = jnp.zeros((rows, block_cols), full)
            dk = jnp.zeros((rows, block_cols), full)
            dv = jnp.zeros((rows, block_cols), full)
            for t in range(block_cols // head_dim):
                h = c * (block_cols // head_dim) + t
                here = jnp.logical_and(block_lane >= t * head_dim, block_lane < (t + 1) * head_dim)
                zero = jnp.zeros_like(q)
                do_h = jnp.where(here, do, zero)
                weights = pb[s * heads + h]
                p = weights.astype(full)
                dp = nt(do_h, v)
                delta = jnp.sum(dp * p, axis=1, keepdims=True)
                ds = (p * (dp - delta)).astype(low)
                bias_sum[h] += ds.astype(full)
                dv = jnp.where(here, tn(weights, do), dv)
                dq = jnp.where(here, jnp.dot(ds, k, preferred_element_type=full), dq)
                dk = jnp.where(here, tn(ds, q), dk)
            dqkv[:, cols] = (dq * scale).astype(low)
            dqkv[:, k_cols] = dk.astype(low)
            dqkv[:, v_cols] = dv.astype(low)
        dqkv_t[:, pl.ds(pl.multiple_of(s * rows, rows), rows)] = dqkv[...].T
        for e in range(exps):
            dn1_send[s, :, e * row_block : (e + 1) * row_block] = jnp.dot(
                dqkv[...], wqkv[e], preferred_element_type=full
            ).astype(low)

        @pl.when(i == 0)
        def _():
            dn1_copies()[0]().start()

        @pl.when(i == 1)
        def _():
            arrived(dn1_in.at[2], dn1_sem.at[RECV, 2])
            dn1_send[s] = (dn1_send[s].astype(full) + dn1_in[2].astype(full)).astype(low)
            dn1_copies()[1]().start()

        @pl.when(i == 2)
        def _():
            dn1_copies()[2]().start()

        return 0

    lax.fori_loop(0, exps, attend_back, 0)
    ys.next(0)

    n1_copy.wait()
    seg = wq_send.shape[2]
    parts = wq_send.shape[1]
    segs = mids.shape[1] - 1
    for e in range(exps):
        part = kept[0:exps, :, e * row_block : (e + 1) * row_block].reshape(exps * rows, row_block)
        total = dot(dqkv_t[...], part)
        for j in range(parts):
            wq_send[e, j] = total[j * seg : (j + 1) * seg].astype(low)

    def owner(j):
        section, within = j // (head_cols // seg), j % (head_cols // seg)
        col = section * width + at.exp * head_cols + within * seg
        block = col // seg
        return block // segs, block % segs

    def mid_place(grp, k, quad):
        return (grp * (segs + 1) + k) * QUAD + quad

    def mid_copy(src, send_sem, rep, k, e):
        dst = mids.at[rep // QUAD, k, at.quad]
        recv = mid_sem.at[mid_place(rep // QUAD, k, at.quad)]
        stays = jnp.logical_and(rep % QUAD == at.quad, e == at.exp)
        return (
            stays,
            functools.partial(send, src, dst, send_sem, recv, (at.grp, rep % QUAD, e)),
            functools.partial(pltpu.make_async_copy, src, dst, recv),
        )

    def wq_copy(i):
        e, j = i // parts, i % parts
        rep, k = owner(j)
        return mid_copy(wq_send.at[e, j], wq_sem.at[i], rep, k, e)

    def og_copy(r):
        return mid_copy(og_send.at[r], og_sem.at[r], r, segs, at.exp)

    def go(copies, act, act_local):
        stays, away, local = copies

        @pl.when(jnp.logical_not(stays))
        def _():
            act(away)

        if act_local:

            @pl.when(stays)
            def _():
                act_local(local)

    def over(count, copies, act, act_local):
        def one(i, _):
            go(copies(i), act, act_local)
            return 0

        lax.fori_loop(0, count, one, 0)

    over(exps * parts, wq_copy, lambda copy: copy().start(), lambda copy: copy().start())
    group_dz.arrive()
    grad = tn(mine[...].reshape(exps * rows, head_cols), dz_all[...].reshape(exps * rows, width))
    for r in range(reps):
        og_send[r] = grad[:, r * out_cols : (r + 1) * out_cols].T.astype(low)
    over(reps, og_copy, lambda copy: copy().start(), lambda copy: copy().start())

    n1_grad = dn1_send[at.exp].astype(full)
    for j in range(2):
        arrived(dn1_in.at[j], dn1_sem.at[RECV, j])
        n1_grad = n1_grad + dn1_in[j].astype(full)
    x = tokens[...].astype(full)
    r1 = lax.rsqrt(jnp.mean(x * x, axis=1, keepdims=True) + eps_norm)
    scaled = n1_grad * gains[0:1, :]
    token_grad[...] = (
        dh1[...] + r1 * scaled - x * (r1 * r1 * r1) * jnp.mean(scaled * x, axis=1, keepdims=True)
    )
    small_send[exps : exps + 1, :] = jnp.sum(n1_grad * x * r1, axis=0, keepdims=True)

    ys.next(1)
    router_rows = lax.dot_general(
        logit_grad, n2_in[...].astype(full), (((0,), (0,)), ((), ())), preferred_element_type=full, precision=highest
    )
    small_send[0:exps, :] = router_rows[0:exps, :]

    flip = jnp.where(row_of((rows, rows)) + lane_of((rows, rows)) == rows - 1, 1.0, 0.0).astype(low)
    diagonals = []
    for h in range(heads):
        high = bias_sum[h].astype(low)
        rest = (bias_sum[h] - high.astype(full)).astype(low)
        flipped = dot(high, flip) + dot(rest, flip)
        square = jnp.concatenate([flipped, jnp.zeros((rows, rows), full)], axis=1)
        turned = pltpu.roll(square, 0, 1, stride=1, stride_axis=0)
        diagonals.append(jnp.sum(turned, axis=0, keepdims=True))
    diagonals = jnp.concatenate(diagonals + [jnp.zeros((8 - heads, span), full)], axis=0)
    in_bucket = jnp.where(bucket_of(rows - 1 - row_of((span, 128))) == lane_of((span, 128)), 1.0, 0.0)
    bias_line = jnp.dot(diagonals, in_bucket, precision=highest, preferred_element_type=full)
    for h in range(heads):
        small_send[exps + 2 : exps + 3, h * 128 : (h + 1) * 128] = bias_line[h : h + 1, :]

    def small_copies():
        return [
            send(
                small_send,
                small_exp.at[at.exp],
                small_sem.at[SEND, exp_peer(k)],
                small_sem.at[RECV, at.exp],
                at.device(at.rep, exp_peer(k)),
            )
            for k in range(1, exps)
        ]

    for copy in small_copies():
        copy.start()
    small_exp[at.exp] = small_send[...]

    def mid_sum(grp, k):
        for q in range(QUAD):
            arrived(mids.at[grp, k, q], mid_sem.at[mid_place(grp, k, q)])
        total = mids[grp, k, 0].astype(full)
        for q in range(1, QUAD):
            total = total + mids[grp, k, q].astype(full)
        return total

    far = 1 - at.grp
    for k in range(segs + 1):
        far_send[k] = mid_sum(far, k).astype(low)

    def far_copy():
        return send(far_send, far_in, far_sem.at[SEND], far_sem.at[RECV], (far, at.quad, at.exp))

    far_copy().start()
    for k in range(1, exps):
        arrived(small_exp.at[exp_peer(k)], small_sem.at[RECV, exp_peer(k)])
    total = small_exp[0]
    for e in range(1, exps):
        total = total + small_exp[e]
    small_sum[...] = total
    for e in range(exps):
        small_sum[exps + 3 + e : exps + 4 + e, :] = small_exp[e, exps + 2 : exps + 3, :]

    def small2_copies():
        return [
            send(
                small_sum,
                small_rep.at[at.quad],
                small2_sem.at[SEND, k - 1],
                small2_sem.at[RECV, at.quad],
                (at.grp, (at.quad + k) % QUAD, at.exp),
            )
            for k in range(1, QUAD)
        ]

    def small3_copy():
        return send(small_half, small_far, small3_sem.at[SEND], small3_sem.at[RECV], (far, at.quad, at.exp))

    for copy in small2_copies():
        copy.start()
    small_rep[at.quad] = small_sum[...]
    for step in range(2, steps):
        ys.next(step)
    length = lengths[at.base]
    for e in range(1, exps):
        length = jnp.where(deal[at.base + e] == at.me, lengths[at.base + e], length)
    block = ys.result()[0]
    block_out[...] = jnp.where(row_of((rows, 1)) < length, block, jnp.zeros_like(block))
    for k in range(1, QUAD):
        arrived(small_rep.at[(at.quad + k) % QUAD], small2_sem.at[RECV, (at.quad + k) % QUAD])
    total = small_rep[0]
    for q in range(1, QUAD):
        total = total + small_rep[q]
    small_half[...] = total
    small3_copy().start()
    arrived(small_far, small3_sem.at[RECV])
    total = small_half[...] + small_far[...]
    small_out[...] = total

    near = [mid_sum(at.grp, k) for k in range(segs + 1)]
    arrived(far_in, far_sem.at[RECV])
    grads = [(near[k] + far_in[k].astype(full)).T for k in range(segs + 1)]
    qkv_grad[...] = jnp.concatenate(grads[:segs], axis=1)
    out_grad[...] = grads[segs]
    for home in homes:
        home.arrive()

    ys.finish()

    for home in homes:
        home.sent()

    over(exps * parts, wq_copy, lambda copy: copy().wait_send(), None)
    over(reps, og_copy, lambda copy: copy().wait_send(), None)
    far_copy().wait_send()
    small3_copy().wait_send()
    for copies in (do_copies(), small_copies(), small2_copies()):
        for copy in copies:
            copy.wait_send()
    for copy in dn1_copies():
        copy().wait_send()
    group_dz.sent()


def routed(routes_t, seq, rows):
    pair = routes_t[:, pl.ds(pl.multiple_of(seq * rows, rows), rows)].astype(full)
    cols = jnp.concatenate([pair, jnp.zeros((126, rows), full)], axis=0).T
    lane = lane_of((rows, 128)).astype(full)
    return jnp.logical_or(lane == cols[:, 0:1], lane == cols[:, 1:2])


def backward_call(
    grps, exps, lengths, deal, y_half, y_far, both_g, down_g, in_before, down_before, n1,
    cot_all, routes_t, tokens, n_total, c_in, n2, probs, h1, qkv, pb, mine, wqkv, wout, gains, router
):
    reps = grps * QUAD
    rows, width = tokens.shape
    heads = HEADS // exps
    head_cols = width // exps
    row_block = wqkv.shape[2]
    out_cols = wout.shape[3]
    shard_cols = 3 * width // reps
    seg = math.gcd(shard_cols, head_cols)
    segs = shard_cols // seg
    parts = 3 * head_cols // seg
    members = QUAD * exps
    chip_bits = bits_of(members) - 1
    small_rows = -(-(2 * exps + 3) // 8) * 8
    shape = jax.ShapeDtypeStruct
    vmem = pl.BlockSpec(memory_space=pltpu.VMEM)
    smem = pl.BlockSpec(memory_space=pltpu.SMEM)
    hbm = pl.BlockSpec(memory_space=pl.ANY)
    results = [
        (shape((rows, width), full), vmem),
        (shape((rows, width), low), vmem),
        (shape(in_before.shape, low), hbm),
        (shape(down_before.shape, low), hbm),
        (shape((row_block, shard_cols), full), vmem),
        (shape((row_block, out_cols), full), vmem),
        (shape((small_rows, width), full), vmem),
    ]
    dma = pltpu.SemaphoreType.DMA
    bufs = [pltpu.VMEM((1 << (chip_bits - s), rows, width), low) for s in range(chip_bits + 1)]
    return pl.pallas_call(
        functools.partial(backward_kernel, grps, exps),
        out_shape=[r[0] for r in results],
        in_specs=[smem] * 2 + [hbm] * 8 + [vmem] * 6 + [hbm] * 6 + [vmem] * 2,
        out_specs=[r[1] for r in results],
        scratch_shapes=[
            pltpu.VMEM(h1.shape, full),
            pltpu.VMEM(qkv.shape, low),
            pltpu.VMEM(pb.shape, low),
            pltpu.VMEM(mine.shape, low),
            pltpu.VMEM(wqkv.shape, low),
            pltpu.VMEM(wout.shape, low),
            pltpu.VMEM((members // 2, rows, width), low),
            list(bufs),
            pltpu.VMEM((rows, width), full),
            pltpu.VMEM((rows, width), low),
            pltpu.VMEM((exps, rows, width), low),
            pltpu.VMEM((exps, rows, head_cols), low),
            pltpu.VMEM((exps, rows, head_cols), low),
            pltpu.VMEM((heads, rows, rows), full),
            pltpu.VMEM((rows, 3 * head_cols), low),
            pltpu.VMEM((3 * head_cols, exps * rows), low),
            pltpu.VMEM((exps, rows, width), low),
            pltpu.VMEM((3, rows, width), low),
            pltpu.VMEM((exps, parts, seg, row_block), low),
            pltpu.VMEM((reps, seg, row_block), low),
            pltpu.VMEM((grps, segs + 1, QUAD, seg, row_block), low),
            pltpu.VMEM((segs + 1, seg, row_block), low),
            pltpu.VMEM((segs + 1, seg, row_block), low),
            pltpu.VMEM((small_rows, width), full),
            pltpu.VMEM((exps, small_rows, width), full),
            pltpu.VMEM((small_rows, width), full),
            pltpu.VMEM((QUAD, small_rows, width), full),
            pltpu.VMEM((small_rows, width), full),
            pltpu.VMEM((small_rows, width), full),
            dma((2, 3 << chip_bits)),
            dma((2,)),
            dma((2, 2, 2 * reps)),
            dma((2, 2, max(QUAD, grps))),
            dma((2, exps)),
            dma((2, exps)),
            dma((2, exps)),
            dma((exps * parts,)),
            dma((reps,)),
            dma((grps * (segs + 1) * QUAD,)),
            dma((2,)),
            dma((2, exps)),
            dma((2, QUAD)),
            dma((2,)),
            dma((2,)),
            dma((6,)),
        ],
        compiler_params=pltpu.CompilerParams(
            collective_id=1, has_side_effects=True, vmem_limit_bytes=60 * 1024 * 1024
        ),
        input_output_aliases={6: 2, 7: 3},
        name="backward",
    )(
        lengths, deal, y_half, y_far, both_g, down_g, in_before, down_before, n1, cot_all,
        routes_t, tokens, n_total, c_in, n2, probs, h1, qkv, pb, mine, wqkv, wout, gains, router
    )


def per_device(
    tokens,
    cotangent,
    seq_lengths,
    deal,
    routes,
    attn_qkv,
    qkv_first,
    qkv_second,
    attn_out,
    out_first,
    out_second,
    rel_bias,
    bias_first,
    bias_second,
    router,
    router_first,
    router_second,
    norm_gains,
    gains_first,
    gains_second,
    expert_in,
    in_first,
    in_second,
    expert_out,
    down_first,
    down_second,
):
    rows, width = tokens.shape
    experts = router.shape[1]
    capacity = (10 * rows + 4 * experts - 1) // (4 * experts)
    exps = lax.axis_size("exp")
    grps = lax.axis_size("grp")
    routes_t = routes.T
    bias_table = rel_bias.T
    (
        both_w, down_w, cot_all, n_all, comb_all, qkv, pb, context_mine, normed_group, wqkv, wout, hidden_one,
        normed_two, router_probs, in_low, down_low,
    ) = forward_call(
        grps, exps, seq_lengths, bias_table, routes_t, tokens, cotangent, norm_gains.T, router.T,
        attn_qkv, attn_out, expert_in[0], expert_out[0],
    )
    n_total, y_half, y_far, c_in, both_g, down_g, in_before, down_before = expert_call(
        grps, exps, capacity, deal, routes_t, comb_all, n_all, cot_all, both_w, down_w, in_low, down_low,
        hidden_one,
    )
    token_grad, block_out, in_parts, down_parts, qkv_grad, out_grad, small = backward_call(
        grps, exps, seq_lengths, deal, y_half, y_far, both_g, down_g,
        in_before, down_before, normed_group, cot_all, routes_t, tokens, n_total, c_in, normed_two, router_probs, hidden_one, qkv, pb, context_mine, wqkv,
        wout, norm_gains.T, router.T,
    )
    states = [
        attn_qkv, qkv_first, qkv_second, attn_out, out_first, out_second, bias_table, bias_first.T, bias_second.T,
        router.T, router_first.T, router_second.T, norm_gains.T, gains_first.T, gains_second.T,
        expert_in[0], in_first[0], in_second[0], expert_out[0], down_first[0], down_second[0],
    ]
    new = list(adam_call(exps, in_parts, down_parts, qkv_grad, out_grad, small, states))
    new = new[:6] + [array.T for array in new[6:15]] + [array[None] for array in new[15:]]
    return (block_out, token_grad, *new)


def bucket_onehot(length):
    places = jnp.arange(length, dtype=jnp.int32)
    offset = places[None, :] - places[:, None]
    distance = jnp.abs(offset)
    bucket = 16 * (offset > 0).astype(jnp.int32)
    for threshold in thresholds:
        bucket = bucket + (distance >= threshold).astype(jnp.int32)
    return (bucket[:, :, None] == jnp.arange(BUCKETS, dtype=jnp.int32)[None, None, :]).astype(full)


def swap(pieces, axes):
    return lax.all_to_all(pieces, axes, split_axis=0, concat_axis=0, tiled=True)


def spread(block, axes):
    members = lax.axis_size(axes)
    return swap(jnp.broadcast_to(block[None], (members,) + block.shape), axes)


def plain_device(
    tokens,
    cotangent,
    seq_lengths,
    deal,
    routes,
    attn_qkv,
    qkv_first,
    qkv_second,
    attn_out,
    out_first,
    out_second,
    rel_bias,
    bias_first,
    bias_second,
    router,
    router_first,
    router_second,
    norm_gains,
    gains_first,
    gains_second,
    expert_in,
    in_first,
    in_second,
    expert_out,
    down_first,
    down_second,
):
    rows, width = tokens.shape
    head_dim = width // HEADS
    score_scale = 1.0 / math.sqrt(head_dim)
    experts = router.shape[1]
    capacity = (10 * rows + 4 * experts - 1) // (4 * experts)
    exps = lax.axis_size("exp")
    grps = lax.axis_size("grp")
    reps = grps * QUAD
    heads = HEADS // exps
    head_cols = heads * head_dim
    place = lax.axis_index("exp")
    base = lax.axis_index(REP) * exps
    me = base + place
    slab = expert_in.shape[1]
    units = expert_out.shape[1]
    quarter = grps * units

    row_block = attn_qkv.shape[0]
    qkv_rows = lax.all_gather(attn_qkv.astype(low), REP, axis=1, tiled=True)
    out_rows = lax.all_gather(attn_out.astype(low), REP, axis=1, tiled=True)
    qkv_pieces = jnp.transpose(
        qkv_rows.reshape(row_block, 3, exps, head_cols), (2, 0, 1, 3)
    ).reshape(exps, row_block, 3 * head_cols)
    qkv_mine = swap(qkv_pieces, "exp").reshape(width, 3 * head_cols)
    full_out = spread(out_rows, "exp").reshape(width, width)

    group_tokens = spread(tokens, "exp")
    group_cotangent = spread(cotangent, "exp")
    my_cotangent = lax.dynamic_index_in_dim(group_cotangent, deal[me] - base, 0, keepdims=False)

    my_routes = lax.dynamic_slice_in_dim(routes, me * rows, rows, 0)
    places = jnp.arange(rows, dtype=jnp.int32)
    valid_rows = (places < seq_lengths[me]).astype(full)
    group_lengths = lax.dynamic_slice_in_dim(seq_lengths, base, exps, 0)
    key_ok = places[None, :] < group_lengths[:, None]
    gain_one = norm_gains[:, 0]
    gain_two = norm_gains[:, 1]

    chosen = (my_routes[:, :, None] == jnp.arange(experts, dtype=jnp.int32)[None, None, :]).astype(full)
    flat_routes = my_routes.reshape(-1)
    route_hot = (flat_routes[:, None] == jnp.arange(experts, dtype=jnp.int32)[None, :]).astype(jnp.int32)
    before = jnp.cumsum(route_hot, axis=0) - route_hot
    slot_index = jnp.sum(before * route_hot, axis=-1)
    target = (flat_routes * capacity + slot_index).reshape(rows, 2)
    slots = experts * capacity
    slot_ids = jnp.arange(slots, dtype=jnp.int32)
    place_first = slot_ids[:, None] == target[None, :, 0]
    place_second = slot_ids[:, None] == target[None, :, 1]
    place_any = jnp.logical_or(place_first, place_second).astype(low)

    shard_in = expert_in[0].astype(low).reshape(slab, 2, grps, QUAD, units)
    in_pieces = jnp.transpose(shard_in, (1, 3, 0, 2, 4)).reshape(2, 1, QUAD, slab, quarter)
    in_pieces = jnp.broadcast_to(in_pieces, (2, grps, QUAD, slab, quarter)).reshape(
        2, reps, slab, quarter
    )
    down_mine = spread(expert_out[0].astype(low), "grp").reshape(quarter, width)
    gate_mine = swap(in_pieces[0], REP).reshape(width, quarter)
    up_mine = swap(in_pieces[1], REP).reshape(width, quarter)

    upstream = my_cotangent.astype(full) * valid_rows[:, None]

    def to_experts(block):
        sent = block.reshape((1, experts) + block.shape[1:])
        sent = jnp.broadcast_to(sent, (QUAD,) + sent.shape[1:])
        return swap(sent.reshape((QUAD * experts,) + block.shape[1:]), PLANE)

    def dispatch(values):
        return dot(place_any, values).astype(low).reshape(experts, capacity, width)

    expert_upstream = to_experts(dispatch(upstream.astype(low))).reshape(-1, width)
    active_grad_bare = lax.dot_general(
        expert_upstream, down_mine, (((1,), (1,)), ((), ())), preferred_element_type=full
    )

    x_group = group_tokens.astype(full)
    scale_group = lax.rsqrt(jnp.mean(x_group * x_group, axis=-1, keepdims=True) + eps_norm)
    normed_group = (x_group * scale_group * gain_one).astype(low).reshape(exps * rows, width)
    qkv = dot(normed_group, qkv_mine).astype(low).reshape(exps, rows, 3, heads, head_dim)
    queries = qkv[:, :, 0]
    key_rows = qkv[:, :, 1]
    values = qkv[:, :, 2]
    onehot = bucket_onehot(rows)
    bias_mine = lax.dynamic_slice_in_dim(rel_bias, place * heads, heads, 1)
    bias_table = jnp.einsum("ijb,bh->hij", onehot, bias_mine, precision=highest)

    def scores_of():
        raw = (
            jnp.einsum("sihd,sjhd->shij", queries, key_rows, preferred_element_type=full)
            * score_scale
            + bias_table[None]
        )
        return jnp.where(key_ok[:, None, None, :], raw, -1e30)

    scores = scores_of()
    row_max = jnp.max(scores, axis=-1, keepdims=True)
    log_total = row_max + jnp.log(jnp.sum(jnp.exp(scores - row_max), axis=-1, keepdims=True))
    weights_low = jnp.exp(scores - log_total).astype(low)
    context_mine = (
        jnp.einsum("shij,sjhd->sihd", weights_low, values, preferred_element_type=full)
        .astype(low)
        .reshape(exps, rows, head_cols)
    )
    context = jnp.transpose(swap(context_mine, "exp"), (1, 0, 2)).reshape(rows, width)

    x_float = tokens.astype(full)
    scale_one = lax.rsqrt(jnp.mean(x_float * x_float, axis=-1, keepdims=True) + eps_norm)
    hidden_one = x_float + dot(context, full_out)
    scale_two = lax.rsqrt(jnp.mean(hidden_one * hidden_one, axis=-1, keepdims=True) + eps_norm)
    normed_two = (hidden_one * scale_two * gain_two).astype(low)
    normed_float = normed_two.astype(full)
    router_probs = jax.nn.softmax(jnp.dot(normed_float, router, precision=highest), axis=-1)
    picked = jnp.sum(router_probs[:, None, :] * chosen, axis=-1)
    gate_total = jnp.sum(picked, axis=-1, keepdims=True)
    gate_value = picked / gate_total
    combine = gate_value * valid_rows[:, None]
    combine_slots = jnp.sum(
        jnp.where(place_first, combine[None, :, 0], 0.0)
        + jnp.where(place_second, combine[None, :, 1], 0.0),
        axis=1,
    ).reshape(experts, 1, capacity)

    expert_rows = to_experts(dispatch(normed_two)).reshape(-1, width)
    expert_combine = to_experts(combine_slots).reshape(-1, 1)

    gate_part = dot(expert_rows, gate_mine)
    up_part = dot(expert_rows, up_mine)
    active_float, active_pull = jax.vjp(gated_unit, gate_part, up_part)
    active = active_float.astype(low)
    active_scaled = (active_float * expert_combine).astype(low)
    combine_grad_part = jnp.sum(active_float * active_grad_bare, axis=-1).reshape(
        QUAD * experts, 1, capacity
    )
    gate_part_grad, up_part_grad = active_pull(active_grad_bare * expert_combine)
    gate_part_grad = gate_part_grad.astype(low)
    up_part_grad = up_part_grad.astype(low)
    rows_grad_part = (
        lax.dot_general(gate_part_grad, gate_mine, (((1,), (1,)), ((), ())), preferred_element_type=full)
        + lax.dot_general(up_part_grad, up_mine, (((1,), (1,)), ((), ())), preferred_element_type=full)
    ).astype(low)
    output_part = dot(active, down_mine).astype(low)

    combine_grad_back = swap(combine_grad_part, PLANE)
    rows_grad_back = swap(rows_grad_part.reshape(QUAD * experts, capacity, width), PLANE)
    output_back = swap(output_part.reshape(QUAD * experts, capacity, width), PLANE)

    def transposed_dot(a, b):
        return lax.dot_general(a, b, (((0,), (0,)), ((), ())), preferred_element_type=full)

    down_grad = transposed_dot(active_scaled, expert_upstream).astype(low)
    gate_grad = transposed_dot(expert_rows, gate_part_grad).astype(low)
    up_grad = transposed_dot(expert_rows, up_part_grad).astype(low)
    down_share = jnp.sum(
        swap(down_grad.reshape(grps, units, width), "grp").astype(full), axis=0
    )[None]

    def in_columns(grad):
        back = swap(grad.reshape(reps, slab, quarter), REP).astype(full)
        back = jnp.sum(back.reshape(grps, QUAD, slab, grps, units), axis=0)
        return jnp.transpose(back, (1, 2, 0, 3)).reshape(slab, grps * QUAD * units)

    in_share = jnp.concatenate([in_columns(gate_grad), in_columns(up_grad)], axis=1)[None]

    def from_slots(placed, parts):
        hot = jnp.broadcast_to(placed.astype(low)[None], (QUAD,) + placed.shape).reshape(-1, rows)
        return lax.dot_general(
            hot, parts.reshape(-1, width), (((0,), (0,)), ((), ())), preferred_element_type=full
        )

    mixture = combine[:, :1] * from_slots(place_first, output_back) + combine[:, 1:] * from_slots(
        place_second, output_back
    )
    block_loader = (valid_rows[:, None] * (hidden_one + mixture)).astype(low)
    seq_ids = jnp.arange(deal.shape[0], dtype=jnp.int32)
    dealt_seq = jnp.sum(jnp.where(deal == me, seq_ids, 0))
    block_out = lax.dynamic_index_in_dim(
        spread(block_loader, "exp"), dealt_seq - base, 0, keepdims=False
    )

    combine_grad_slots = jnp.sum(combine_grad_back.reshape(QUAD, slots), axis=0)
    combine_grad = jnp.stack(
        [
            jnp.sum(jnp.where(place_first, combine_grad_slots[:, None], 0.0), axis=0),
            jnp.sum(jnp.where(place_second, combine_grad_slots[:, None], 0.0), axis=0),
        ],
        axis=1,
    )
    gate_grad_value = combine_grad * valid_rows[:, None]
    picked_grad = (
        gate_grad_value - jnp.sum(gate_grad_value * gate_value, axis=-1, keepdims=True)
    ) / gate_total
    probs_grad = jnp.sum(picked_grad[:, :, None] * chosen, axis=1)
    logit_grad = router_probs * (
        probs_grad - jnp.sum(probs_grad * router_probs, axis=-1, keepdims=True)
    )
    router_grad = jnp.dot(normed_float.T, logit_grad, precision=highest)
    normed_grad = jnp.dot(logit_grad, router.T, precision=highest) + from_slots(
        jnp.logical_or(place_first, place_second), rows_grad_back
    )
    scaled_two = normed_grad * gain_two
    hidden_grad = (
        upstream
        + scale_two * scaled_two
        - hidden_one * scale_two**3 * jnp.mean(scaled_two * hidden_one, axis=-1, keepdims=True)
    )
    gain_two_grad = jnp.sum(normed_grad * hidden_one * scale_two, axis=0)
    branch_grad = hidden_grad.astype(low)
    context_grad = lax.dot_general(
        branch_grad, full_out, (((1,), (1,)), ((), ())), preferred_element_type=full
    ).astype(low)
    context_grad_pieces = jnp.transpose(context_grad.reshape(rows, exps, head_cols), (1, 0, 2))
    context_grad_mine = swap(context_grad_pieces, "exp").reshape(exps, rows, heads, head_dim)
    branch_group = spread(branch_grad, "exp").reshape(exps * rows, width)
    out_grad = transposed_dot(context_mine.reshape(exps * rows, head_cols), branch_group).astype(low)

    scores = scores_of()
    probs_again = jnp.exp(scores - log_total)
    weights_again = probs_again.astype(low)
    values_grad = jnp.einsum(
        "shij,sihd->sjhd", weights_again, context_grad_mine, preferred_element_type=full
    )
    probs_grad_att = jnp.einsum(
        "sihd,sjhd->shij", context_grad_mine, values, preferred_element_type=full
    )
    row_delta = jnp.sum(probs_grad_att * probs_again, axis=-1, keepdims=True)
    scores_grad = (probs_again * (probs_grad_att - row_delta)).astype(low)
    scores_grad_sum = jnp.sum(scores_grad.astype(full), axis=0)
    bias_grad_mine = jnp.einsum("hij,ijb->bh", scores_grad_sum, onehot, precision=highest)
    bias_grad = lax.dynamic_update_slice_in_dim(
        jnp.zeros((BUCKETS, HEADS), full), bias_grad_mine, place * heads, 1
    )
    queries_grad = (
        jnp.einsum("shij,sjhd->sihd", scores_grad, key_rows, preferred_element_type=full)
        * score_scale
    )
    keys_grad = (
        jnp.einsum("shij,sihd->sjhd", scores_grad, queries, preferred_element_type=full)
        * score_scale
    )
    qkv_grad = (
        jnp.stack([queries_grad, keys_grad, values_grad], axis=2)
        .astype(low)
        .reshape(exps * rows, 3 * head_cols)
    )
    normed_one_part = lax.dot_general(
        qkv_grad, qkv_mine, (((1,), (1,)), ((), ())), preferred_element_type=full
    ).astype(low)
    normed_one_grad = jnp.sum(
        swap(normed_one_part.reshape(exps, rows, width), "exp").astype(full), axis=0
    )
    scaled_one = normed_one_grad * gain_one
    token_grad = (
        hidden_grad
        + scale_one * scaled_one
        - x_float * scale_one**3 * jnp.mean(scaled_one * x_float, axis=-1, keepdims=True)
    )
    gain_one_grad = jnp.sum(normed_one_grad * x_float * scale_one, axis=0)

    qkv_weight_grad = transposed_dot(normed_group, qkv_grad).astype(low)
    qkv_grad_rows = swap(qkv_weight_grad.reshape(exps, row_block, 3 * head_cols), "exp")
    qkv_grad_rows = jnp.transpose(
        qkv_grad_rows.reshape(exps, row_block, 3, head_cols), (1, 2, 0, 3)
    ).reshape(row_block, reps, -1)
    qkv_share = jnp.sum(
        swap(jnp.transpose(qkv_grad_rows, (1, 0, 2)), REP).astype(full), axis=0
    )
    out_pieces = jnp.transpose(out_grad.reshape(row_block, reps, -1), (1, 0, 2))
    out_share = jnp.sum(swap(out_pieces, REP).astype(full), axis=0)

    small = jnp.concatenate(
        [
            router_grad.reshape(-1),
            jnp.stack([gain_one_grad, gain_two_grad], axis=1).reshape(-1),
            bias_grad.reshape(-1),
        ]
    ).reshape(-1, 128)
    small_total = jnp.sum(lax.all_gather(small, ALL, axis=0, tiled=False), axis=0).reshape(-1)
    router_total = small_total[: router.size].reshape(router.shape)
    gains_total = small_total[router.size : router.size + norm_gains.size].reshape(norm_gains.shape)
    bias_total = small_total[router.size + norm_gains.size :].reshape(rel_bias.shape)

    qkv_new = adamw_update(attn_qkv, qkv_first, qkv_second, qkv_share, 1.5 / math.sqrt(D), 0.1)
    out_new = adamw_update(attn_out, out_first, out_second, out_share, 6.0 / math.sqrt(D), 0.1)
    bias_new = adamw_update(rel_bias, bias_first, bias_second, bias_total, 0.3, 0.0)
    router_new = adamw_update(
        router, router_first, router_second, router_total, 1.0 / math.sqrt(D), 0.1
    )
    gains_new = adamw_update(norm_gains, gains_first, gains_second, gains_total, 0.5, 0.0)
    in_new = adamw_update(expert_in, in_first, in_second, in_share, 1.5 / math.sqrt(D), 0.1)
    down_new = adamw_update(
        expert_out, down_first, down_second, down_share, 1.5 / math.sqrt(FF), 0.1
    )
    return (
        (block_out, token_grad)
        + qkv_new
        + out_new
        + bias_new
        + router_new
        + gains_new
        + in_new
        + down_new
    )


def solution(mesh):
    reps, exps = mesh.devices.shape
    split = Mesh(mesh.devices.reshape(reps // QUAD, QUAD, exps), ALL)
    by_rows = P(ALL, None)
    attn = P("exp", REP)
    expert = P("exp", REP, None)
    return jax.shard_map(
        per_device if (reps, exps) == (2 * QUAD, 4) else plain_device,
        mesh=split,
        in_specs=(by_rows, by_rows) + (P(),) * 3 + (attn,) * 6 + (P(),) * 9 + (expert,) * 6,
        out_specs=(by_rows, by_rows) + (attn,) * 6 + (P(),) * 9 + (expert,) * 6,
        check_vma=False,
    )
```

```python
import functools
import math

import jax
import jax.numpy as jnp
from jax import lax
from jax.experimental import pallas as pl
from jax.experimental.pallas import tpu as pltpu
from jax.sharding import Mesh
from jax.sharding import PartitionSpec as P

D = 1024
HEADS = 16
FF = 2816
BUCKETS = 32
STEP = 10
QUAD = 4
REP = ("grp", "quad")
PLANE = ("quad", "exp")
ALL = ("grp", "quad", "exp")

highest = lax.Precision.HIGHEST
eps_norm = 1e-06
thresholds = (1, 2, 3, 4, 5, 6, 7, 8, 11, 16, 22, 32, 45, 64, 90)
beta_one = 0.9
beta_two = 0.999
eps_adam = 1e-08
low = jnp.bfloat16
full = jnp.float32
MESH = pl.DeviceIdType.MESH


def adamw_update(weight, moment, second, gradient, step_rate, decay_factor):
    new_moment = beta_one * moment + (1.0 - beta_one) * gradient
    new_second = beta_two * second + (1.0 - beta_two) * gradient * gradient
    corrected = new_moment / (1.0 - beta_one**STEP)
    scaled = new_second / (1.0 - beta_two**STEP)
    new_weight = weight - step_rate * (
        corrected / (jnp.sqrt(scaled) + eps_adam) + decay_factor * weight
    )
    return (new_moment, new_second, new_weight)


def gated_unit(gate_input, up_input):
    return jax.nn.gelu(gate_input, approximate=True) * up_input


def dot(a, b):
    return jnp.dot(a, b, preferred_element_type=full)


def nt(a, b, precision=None):
    return lax.dot_general(a, b, (((1,), (1,)), ((), ())), preferred_element_type=full, precision=precision)


def tn(a, b):
    return lax.dot_general(a, b, (((0,), (0,)), ((), ())), preferred_element_type=full)


class Where:
    def __init__(self, grps, exps):
        self.grps, self.exps = grps, exps
        self.reps = grps * QUAD
        self.grp = lax.axis_index("grp")
        self.quad = lax.axis_index("quad")
        self.exp = lax.axis_index("exp")
        self.rep = self.grp * QUAD + self.quad
        self.base = self.rep * exps
        self.me = self.base + self.exp

    def device(self, rep, exp):
        return (rep // QUAD, rep % QUAD, exp)

    def near(self, flip):
        q = self.quad
        if flip & 1:
            q = q + 1 - 2 * (q % 2)
        if flip & 2:
            q = q + 2 - 4 * (q // 2)
        return q


def send(src, dst, send_sem, recv_sem, device):
    return pltpu.make_async_remote_copy(
        src_ref=src, dst_ref=dst, send_sem=send_sem, recv_sem=recv_sem, device_id=device, device_id_type=MESH
    )


def arrived(ref, sem):
    pltpu.make_async_copy(ref, ref, sem).wait()


def greet(count, device):
    barrier = pltpu.get_barrier_semaphore()

    def one(k, _):
        pl.semaphore_signal(barrier, inc=1, device_id=device(k), device_id_type=MESH)
        return 0

    lax.fori_loop(1, count + 1, one, 0)
    return functools.partial(pl.semaphore_wait, barrier, count)


def everyone(at):
    count = at.reps * at.exps

    def device(k):
        other = (at.me + k) % count
        return at.device(other // at.exps, other % at.exps)

    return count - 1, device


def neighbours(at):
    members = QUAD * at.exps
    plane = at.quad * at.exps + at.exp

    def device(k):
        other = (plane + k) % members
        rest = k - members
        grp = jnp.where(k < members, at.grp, (at.grp + 1 + rest // QUAD) % at.grps)
        quad = jnp.where(k < members, other // at.exps, rest % QUAD)
        return grp, quad, jnp.where(k < members, other % at.exps, at.exp)

    return members - 1 + QUAD * (at.grps - 1), device


def turn(exp, i):
    beside = exp + 1 - 2 * (exp % 2)
    return jnp.where(i == 0, (beside + 2) % 4, jnp.where(i == 1, (exp + 2) % 4, jnp.where(i == 2, beside, exp)))


def lane_of(shape):
    return lax.broadcasted_iota(jnp.int32, shape, 1)


def row_of(shape):
    return lax.broadcasted_iota(jnp.int32, shape, 0)


def bucket_of(offset):
    distance = jnp.abs(offset)
    bucket = jnp.where(offset > 0, 16, 0)
    for threshold in thresholds:
        bucket = bucket + jnp.where(distance >= threshold, 1, 0)
    return bucket


def bits_of(count):
    return count.bit_length() - 1


def column_parts(width):
    tiles = width // 128
    cuts = [0, (tiles + 2) // 3, (2 * tiles + 2) // 3, tiles]
    return [(cuts[i] * 128, (cuts[i + 1] - cuts[i]) * 128) for i in range(3)]


def flipped(place, bit):
    return place + (1 - 2 * ((place // (1 << bit)) % 2)) * (1 << bit)


class Doubling:
    def __init__(self, at, own, every, sems, core_sems, orders):
        self.at, self.own, self.every = at, own, every
        self.sems, self.core_sems, self.orders = sems, core_sems, orders
        self.plane = at.quad * at.exps + at.exp
        self.steps = len(orders[0])
        self.parts = column_parts(own.shape[1])

    def device(self, bit):
        other = flipped(self.plane, bit)
        return (self.at.grp, other // self.at.exps, other % self.at.exps)

    def place(self, part, j):
        p = self.plane
        for i, bit in enumerate(self.orders[part]):
            if (j >> i) & 1:
                p = flipped(p, bit + 1)
        return p

    def block(self, part, p):
        begin, size = self.parts[part]
        return self.every.at[p, :, pl.ds(begin, size)]

    def source(self, part, j):
        begin, size = self.parts[part]
        return self.own.at[:, pl.ds(begin, size)] if j == 0 else self.block(part, self.place(part, j))

    def index(self, step, part, j):
        return part * (1 << self.steps) + (1 << step) - 1 + j

    def copy(self, step, part, j):
        i = self.index(step, part, j)
        return send(
            self.source(part, j),
            self.block(part, self.place(part, j)),
            self.sems.at[0, i],
            self.sems.at[1, i],
            self.device(self.orders[part][step] + 1),
        )

    def core_copy(self, part, j):
        i = part * (1 << self.steps) + j
        return send(
            self.source(part, j),
            self.block(part, self.place(part, j)),
            self.core_sems.at[0, i],
            self.core_sems.at[1, i],
            self.device(0),
        )

    def start(self):
        for part in range(3):
            for step in range(self.steps):
                self.copy(step, part, 0).start()
        for part in range(3):
            self.core_copy(part, 0).start()
        self.keep().start()

    def keep(self):
        return pltpu.make_async_copy(self.own, self.every.at[self.plane], self.core_sems.at[1, 3 << self.steps])

    def next(self, step):
        for part in range(3):
            for j in range(1 << step):
                k = (1 << step) + j
                arrived(self.block(part, self.place(part, k)), self.sems.at[1, self.index(step, part, j)])
                for later in range(step + 1, self.steps):
                    self.copy(later, part, k).start()
                self.core_copy(part, k).start()

    def finish_in(self):
        for part in range(3):
            for j in range(1 << self.steps):
                there = self.block(part, flipped(self.place(part, j), 0))
                arrived(there, self.core_sems.at[1, part * (1 << self.steps) + j])
        self.keep().wait()

    def finish_out(self):
        for part in range(3):
            for j in range(1 << self.steps):
                self.core_copy(part, j).wait_send()
            for step in range(self.steps):
                for j in range(1 << step):
                    self.copy(step, part, j).wait_send()


class Halving:
    def __init__(self, at, bufs, sems, orders):
        self.at, self.bufs, self.sems = at, bufs, sems
        self.plane = at.quad * at.exps + at.exp
        self.places = bits_of(QUAD * at.exps)
        self.chip_bits = list(range(self.places - 1))
        self.parts = column_parts(bufs[0].shape[2])
        self.orders = orders

    def device(self, bit):
        other = flipped(self.plane, bit)
        return (self.at.grp, other // self.at.exps, other % self.at.exps)

    def hop(self, step, part):
        order = self.orders[part]
        bit = order[step]
        left = [b for b in self.chip_bits if b not in order[:step]]
        pos = left.index(bit)
        half = 1 << (len(left) - 1)
        mine = (self.plane // (1 << (bit + 1))) % 2
        device = self.device(bit + 1)
        begin, size = self.parts[part]
        cols = pl.ds(begin, size)
        base = self.base(step, part)

        def index(j, value):
            return (j >> pos) * (1 << (pos + 1)) + value * (1 << pos) + j % (1 << pos)

        pairs = []
        for j in range(half):
            copy = functools.partial(
                send,
                self.bufs[step].at[index(j, 1 - mine), :, cols],
                self.bufs[step + 1].at[j, :, cols],
                self.sems.at[0, base + j],
                self.sems.at[1, base + j],
                device,
            )
            pairs.append((copy, index(j, mine), j))
        return pairs, begin, size, base

    def base(self, step, part):
        n = len(self.chip_bits)
        return part * (1 << n) + sum(1 << (n - 1 - s) for s in range(step))

    def start(self, step, part=None):
        for p in range(3) if part is None else [part]:
            for copy, _, _ in self.hop(step, p)[0]:
                copy().start()

    def add(self, step, part):
        pairs, begin, size, base = self.hop(step, part)
        cols = pl.ds(begin, size)
        here, there = self.bufs[step], self.bufs[step + 1]
        for _, keep, j in pairs:
            arrived(there.at[j, :, cols], self.sems.at[1, base + j])
            there[j, :, begin : begin + size] = (
                there[j, :, begin : begin + size] + here[keep, :, begin : begin + size]
            )

    def next(self, step):
        for p in range(3):
            self.add(step, p)
            if step + 1 < len(self.chip_bits):
                self.start(step + 1, p)

    def result(self):
        return self.bufs[len(self.chip_bits)]

    def finish(self):
        for step in range(len(self.chip_bits)):
            for p in range(3):
                for copy, _, _ in self.hop(step, p)[0]:
                    copy().wait_send()


class Group:
    def __init__(self, at, own, every, sems):
        self.at, self.own, self.every, self.sems = at, own, every, sems
        self.beside, self.across = at.exp + 1 - 2 * (at.exp % 2), (at.exp + 2) % 4

    def copy(self, src, index, send_index, device):
        return send(
            src, self.every.at[index], self.sems.at[0, send_index], self.sems.at[1, index], self.at.device(self.at.rep, device)
        )

    def first(self):
        return [
            self.copy(self.own, self.at.exp, 0, self.across),
            self.copy(self.own, self.at.exp, 1, self.beside),
        ]

    def second(self):
        return self.copy(self.every.at[self.across], self.across, 2, self.beside)

    def start(self):
        for copy in self.first():
            copy.start()

    def pass_on(self):
        arrived(self.every.at[self.across], self.sems.at[1, self.across])
        self.second().start()

    def arrive(self):
        for index in (self.beside, (self.beside + 2) % 4):
            arrived(self.every.at[index], self.sems.at[1, index])

    def sent(self):
        for copy in self.first() + [self.second()]:
            copy.wait_send()


class Tiles:
    def __init__(self, units, reps):
        self.units = units
        self.reps = reps
        self.hidden = units * reps
        self.half = self.hidden // 256
        self.wide = (self.half + 1) // 2
        self.count = 3
        self.size = 128 * self.wide // self.count
        self.skip = 128 * (2 * self.wide - self.half)

    def start(self, quad):
        return 128 * (self.half * (quad // 2) + (self.half - self.wide) * (quad % 2))

    def rows(self, tile):
        result = []
        for k in range(QUAD):
            found = None
            for parity in range(2):
                first = self.start(parity) + tile * self.size
                live = first + (self.skip if parity and tile == 0 else 0)
                begin = max(live, k * self.units)
                end = min(first + self.size, (k + 1) * self.units)
                if end > begin:
                    found = (begin - k * self.units, end - begin, parity, begin - first)
            result.append(found)
        return result


class Outward:
    def __init__(self, at, tiles, tile, in_low, down_slab, both_w, down_w, nothing, sems, down_sems):
        self.at, self.tiles, self.tile = at, tiles, tile
        self.in_low, self.down_slab, self.both_w, self.down_w = in_low, down_slab, both_w, down_w
        self.nothing, self.sems, self.down_sems = nothing, sems, down_sems
        self.slab = in_low.shape[0]

    def source(self, quad, section):
        begin = section * self.tiles.hidden + self.tiles.start(quad) + self.tile * self.tiles.size
        return self.in_low.at[:, pl.ds(pl.multiple_of(begin, 128), self.tiles.size)]

    def target(self, rep, section):
        rows = pl.ds(pl.multiple_of(rep * self.slab, self.slab), self.slab)
        return self.both_w.at[rows, pl.ds(section * self.tiles.size, self.tiles.size)]

    def over(self, act, first=1, last=None):
        at = self.at

        def one(k, _):
            other = (at.rep + k) % at.reps
            for section in range(2):
                act(
                    functools.partial(
                        send,
                        self.source(other % QUAD, section),
                        self.target(at.rep, section),
                        self.sems.at[0, section * at.reps + other],
                        self.sems.at[1, section * at.reps + at.rep],
                        at.device(other, at.exp),
                    )
                )
            return 0

        lax.fori_loop(first, last or at.reps, one, 0)

    def over_down(self, act, act_local):
        at = self.at
        for k, piece in enumerate(self.tiles.rows(self.tile)):
            if piece is None:
                continue
            begin, count, parity, to = piece
            quad = 2 * (at.rep // QUAD) + parity
            src, dst = self.down_slab.at[pl.ds(begin, count)], self.down_w.at[pl.ds(to, count)]
            recv = self.down_sems.at[1, at.rep]
            for g in range(at.grps):
                stays = jnp.logical_and(at.grp == g, at.quad == quad)
                ours = at.rep % QUAD == k

                @pl.when(jnp.logical_and(ours, jnp.logical_not(stays)))
                def _():
                    act(functools.partial(send, src, dst, self.down_sems.at[0, g], recv, (g, quad, at.exp)))

                @pl.when(jnp.logical_and(ours, stays))
                def _():
                    act_local(functools.partial(pltpu.make_async_copy, src, dst, recv))

    def blank(self):
        return pltpu.make_async_copy(
            self.nothing, self.down_w.at[pl.ds(0, self.tiles.skip)], self.down_sems.at[1, self.at.reps]
        )

    def start(self, first=1, last=None):
        at = self.at
        self.over(lambda copy: copy().start(), first, last)
        if first > 1:
            return
        self.over_down(lambda copy: copy().start(), lambda copy: copy().start())
        for section in range(2):
            pltpu.make_async_copy(
                self.source(at.quad, section), self.target(at.rep, section), self.sems.at[1, section * at.reps + at.rep]
            ).start()
        if self.tile == 0:

            @pl.when(at.quad % 2 == 1)
            def _():
                self.blank().start()

    def arrive(self):
        at = self.at

        def one(rep, _):
            for section in range(2):
                arrived(self.target(rep, section), self.sems.at[1, section * at.reps + rep])
            return 0

        lax.fori_loop(0, at.reps, one, 0)
        for parity in range(2):

            @pl.when(at.quad % 2 == parity)
            def _():
                for k, piece in enumerate(self.tiles.rows(self.tile)):
                    if piece is not None and piece[2] == parity:
                        source = QUAD * (at.quad // 2) + k
                        arrived(self.down_w.at[pl.ds(piece[3], piece[1])], self.down_sems.at[1, source])
                if parity and self.tile == 0:
                    self.blank().wait()

    def sent(self):
        self.over(lambda copy: copy().wait_send())
        self.over_down(lambda copy: copy().wait_send(), lambda copy: None)


class Homeward:
    def __init__(self, at, tiles, tile, both, down, in_parts, down_parts, sems, down_sems, sections=(0, 1)):
        self.at, self.tiles, self.tile, self.sections = at, tiles, tile, sections
        self.both, self.down, self.in_parts, self.down_parts = both, down, in_parts, down_parts
        self.sems, self.down_sems = sems, down_sems
        self.slab = in_parts.shape[1]

    def target(self, grp, quad, parity, section):
        skip = self.tiles.skip if parity and self.tile == 0 else 0
        to = section * self.tiles.hidden + self.tiles.start(quad) + self.tile * self.tiles.size + skip
        to = to if isinstance(to, int) else pl.multiple_of(to, 128)
        return skip, self.in_parts.at[grp, :, pl.ds(to, self.tiles.size - skip)]

    def copy(self, rep, parity, section, local=False):
        at = self.at
        skip, dst = self.target(at.grp, at.quad, parity, section)
        rows = pl.ds(pl.multiple_of(rep * self.slab, self.slab), self.slab)
        src = self.both.at[rows, pl.ds(section * self.tiles.size + skip, self.tiles.size - skip)]
        recv = self.sems.at[1, section * at.reps + at.rep]
        if local:
            return pltpu.make_async_copy(src, dst, recv)
        return send(src, dst, self.sems.at[0, section * at.reps + rep], recv, at.device(rep, at.exp))

    def over(self, act, act_local):
        at = self.at
        for parity in range(2):

            @pl.when(at.quad % 2 == parity)
            def _():
                def one(k, _):
                    for section in self.sections:
                        act(self.copy((at.rep + k) % at.reps, parity, section))
                    return 0

                lax.fori_loop(1, at.reps, one, 0)
                if act_local:
                    for section in self.sections:
                        act_local(self.copy(at.rep, parity, section, local=True))

    def over_down(self, act, act_local):
        at = self.at
        if self.down is None:
            return
        for k, piece in enumerate(self.tiles.rows(self.tile)):
            if piece is None:
                continue
            begin, count, parity, to = piece
            src, dst = self.down.at[pl.ds(to, count)], self.down_parts.at[at.grp, pl.ds(begin, count)]
            recv = self.down_sems.at[1, at.grp]
            stays = jnp.logical_and(at.grp == at.quad // 2, at.quad == k)
            ours = at.quad % 2 == parity

            @pl.when(jnp.logical_and(ours, jnp.logical_not(stays)))
            def _():
                act(functools.partial(send, src, dst, self.down_sems.at[0, k], recv, (at.quad // 2, k, at.exp)))

            @pl.when(jnp.logical_and(ours, stays))
            def _():
                act_local(functools.partial(pltpu.make_async_copy, src, dst, recv))

    def start(self):
        self.over_down(lambda copy: copy().start(), lambda copy: copy().start())
        self.over(lambda copy: copy.start(), lambda copy: copy.start())

    def arrive(self):
        at = self.at
        for rep in range(at.reps):
            for section in self.sections:
                _, dst = self.target(rep // QUAD, rep % QUAD, rep % 2, section)
                arrived(dst, self.sems.at[1, section * at.reps + rep])
        for k, piece in enumerate(self.tiles.rows(self.tile)):
            if piece is None or self.down is None:
                continue

            @pl.when(at.quad == k)
            def _():
                for g in range(at.grps):
                    arrived(self.down_parts.at[g, pl.ds(piece[0], piece[1])], self.down_sems.at[1, g])

    def sent(self):
        self.over(lambda copy: copy.wait_send(), None)
        self.over_down(lambda copy: copy().wait_send(), lambda copy: None)


def forward_kernel(
    grps,
    exps,
    lengths,
    bias_table,
    routes_t,
    tokens,
    cotangent,
    gains,
    router,
    attn_qkv,
    attn_out,
    expert_in,
    expert_out,
    both_w,
    down_w,
    cot_all,
    n_all,
    comb_all,
    qkv_out,
    pb_out,
    mine_out,
    n1_out,
    wqkv_out,
    wout_out,
    h1_out,
    n2_out,
    probs_out,
    in_out,
    down_out,
    in_wide,
    down_wide,
    qkv_t,
    out_w,
    in_low,
    down_slab,
    tok_all,
    wqkv,
    wout,
    n1,
    qkv,
    pb,
    mine,
    ctx,
    bias,
    comb_send,
    nothing,
    tok_sem,
    wq_sem,
    wo_sem,
    wo2_sem,
    weight_sem,
    down_sem,
    ctx_sem,
    cot_sem,
    cot_core_sem,
    n_sem,
    n_core_sem,
    comb_sem,
    store_sem,
    cast_sem,
):
    at = Where(grps, exps)
    reps = at.reps
    rows, width = tokens.shape
    heads = HEADS // exps
    head_dim = width // HEADS
    head_cols = heads * head_dim
    block_cols = min(128, head_cols)
    shard_cols, row_block = qkv_t.shape
    seg = math.gcd(shard_cols, head_cols)
    segs = shard_cols // seg
    tiles = Tiles(down_slab.shape[0], reps)
    plane = at.quad * exps + at.exp
    members = QUAD * exps
    scale = 1.0 / math.sqrt(head_dim)
    SEND, RECV = 0, 1

    met = greet(*everyone(at))
    wide_copies = [
        pltpu.make_async_copy(expert_in, in_wide, cast_sem.at[0]),
        pltpu.make_async_copy(expert_out, down_wide, cast_sem.at[1]),
    ]
    for copy in wide_copies:
        copy.start()
    qkv_t[...] = attn_qkv[...].T.astype(low)
    out_w[...] = attn_out[...].astype(low)
    met()

    def exp_peer(k):
        return (at.exp + k) % exps

    group_tokens = Group(at, tokens, tok_all, tok_sem)
    group_tokens.start()
    tok_all[at.exp] = tokens[...]

    def segment(k):
        col = (at.rep * segs + k) * seg
        section = col // width
        within = col - section * width
        owner = within // head_cols
        return owner, section * head_cols + within - owner * head_cols

    def segment_copy(k, shift):
        owner, offset = segment(k)
        src = qkv_t.at[pl.ds(k * seg, seg)]
        dst = wqkv.at[at.exp, pl.ds(pl.multiple_of(offset, seg), seg)]
        target = at.device((at.rep + shift) % reps, owner)
        return owner, src, dst, functools.partial(
            send, src, dst, wq_sem.at[SEND, k * reps + shift], wq_sem.at[RECV, at.exp * 3 * (head_cols // seg) + offset // seg], target
        )

    def over_segments(act, act_local):
        def one(i, _):
            k, shift = i // reps, i % reps
            owner, src, dst, copy = segment_copy(k, shift)
            stays = jnp.logical_and(shift == 0, owner == at.exp)

            @pl.when(jnp.logical_not(stays))
            def _():
                act(copy())

            @pl.when(stays)
            def _():
                act_local(k, src, dst)

            return 0

        lax.fori_loop(0, segs * reps, one, 0)

    def local_segment(k, src, dst):
        _, offset = segment(k)
        pltpu.make_async_copy(src, dst, wq_sem.at[RECV, at.exp * 3 * (head_cols // seg) + offset // seg]).start()

    over_segments(lambda copy: copy.start(), local_segment)

    for k in range(1, reps):
        other = (at.rep + k) % reps
        send(
            out_w, wout.at[at.exp, at.rep], wo_sem.at[SEND, other], wo_sem.at[RECV, at.rep], at.device(other, at.exp)
        ).start()
    wout[at.exp, at.rep] = out_w[...]
    chip_bits = list(range(bits_of(members) - 1))
    cots = Doubling(at, cotangent, cot_all, cot_sem, cot_core_sem, [chip_bits[::-1]] * 3)
    cots.start()

    span = 2 * rows
    bucket = bucket_of(lane_of((8, span)) - rows)
    for h in range(heads):
        line = jnp.zeros((8, span), full)
        for b in range(BUCKETS):
            line = jnp.where(bucket == b, bias_table[at.exp * heads + h, b], line)
        whole = jnp.broadcast_to(line[0:1], (rows, span))
        bias[h] = pltpu.roll(whole, 0, 1, stride=1, stride_axis=0)[:, rows:]

    group_tokens.pass_on()
    group_tokens.arrive()

    def norm_group(s, _):
        x = tok_all[s].astype(full)
        r = lax.rsqrt(jnp.mean(x * x, axis=1, keepdims=True) + eps_norm)
        n1[s] = (x * r * gains[0:1, :]).astype(low)
        return 0

    lax.fori_loop(0, exps, norm_group, 0)

    for copy in wide_copies:
        copy.wait()
    in_low[...] = in_wide[...].astype(low)
    down_slab[...] = down_wide[...].astype(low)
    nothing[...] = jnp.zeros_like(nothing)
    weights = [
        Outward(
            at, tiles, t, in_low, down_slab, both_w.at[t], down_w.at[t], nothing, weight_sem.at[t], down_sem.at[t]
        )
        for t in range(2)
    ]

    weights[0].start()

    def wait_segment(i, _):
        e, j = i // (3 * head_cols // seg), i % (3 * head_cols // seg)
        arrived(wqkv.at[e, pl.ds(pl.multiple_of(j * seg, seg), seg)], wq_sem.at[RECV, i])
        return 0

    lax.fori_loop(0, exps * 3 * head_cols // seg, wait_segment, 0)

    def project(s, _):
        total = jnp.zeros((rows, 3 * head_cols), full)
        for e in range(exps):
            total = total + nt(n1[s, :, e * row_block : (e + 1) * row_block], wqkv[e])
        qkv[s] = total.astype(low)
        return 0

    lax.fori_loop(0, exps, project, 0)

    group_wout = Group(at, wout.at[at.exp], wout, wo2_sem)

    def beside(k):
        if k == 1:
            for j in range(1, reps):
                other = (at.rep + j) % reps
                arrived(wout.at[at.exp, other], wo_sem.at[RECV, other])
            group_wout.start()
        elif k == 2:
            cots.next(0)
        else:
            group_wout.pass_on()

    def attend(i, _):
        s = turn(at.exp, i)
        for k in range(1, exps):

            @pl.when(i == k)
            def _():
                beside(k)

        ok = lane_of((rows, rows)) < lengths[at.base + s]
        lane = lane_of((rows, block_cols))
        for c in range(head_cols // block_cols):
            cols = slice(c * block_cols, (c + 1) * block_cols)
            q = qkv[s, :, cols] * scale
            k = qkv[s, :, head_cols + c * block_cols : head_cols + (c + 1) * block_cols]
            v = qkv[s, :, 2 * head_cols + c * block_cols : 2 * head_cols + (c + 1) * block_cols]
            result = jnp.zeros((rows, block_cols), full)
            for t in range(block_cols // head_dim):
                h = c * (block_cols // head_dim) + t
                here = jnp.logical_and(lane >= t * head_dim, lane < (t + 1) * head_dim)
                scores = nt(jnp.where(here, q, jnp.zeros_like(q)), k) + bias[h]
                scores = jnp.where(ok, scores, -1e30)
                top = jnp.max(scores, axis=1, keepdims=True)
                weights = jnp.exp(scores - top)
                total = jnp.sum(weights, axis=1, keepdims=True)
                weights = (weights * (1.0 / total)).astype(low)
                result = jnp.where(here, jnp.dot(weights, v, preferred_element_type=full), result)
                pb[s * heads + h] = weights
            mine[s, :, cols] = result.astype(low)

        @pl.when(i < exps - 1)
        def _():
            send(
                mine.at[s], ctx.at[at.exp], ctx_sem.at[SEND, s], ctx_sem.at[RECV, at.exp], at.device(at.rep, s)
            ).start()

        @pl.when(i == exps - 1)
        def _():
            pltpu.make_async_copy(mine.at[s], ctx.at[at.exp], ctx_sem.at[RECV, at.exp]).start()

        return 0

    lax.fori_loop(0, exps, attend, 0)

    cots.next(1)
    group_wout.arrive()
    for e in range(exps):
        arrived(ctx.at[e], ctx_sem.at[RECV, e])

    out_cols = wout.shape[3]
    for r in range(reps):
        cols = slice(r * out_cols, (r + 1) * out_cols)
        total = tokens[:, cols].astype(full)
        for e in range(exps):
            total = total + jnp.dot(ctx[e], wout[e, r], preferred_element_type=full)
        h1_out[:, cols] = total
    h1 = h1_out[...]
    r2 = lax.rsqrt(jnp.mean(h1 * h1, axis=1, keepdims=True) + eps_norm)
    n2 = (h1 * r2 * gains[1:2, :]).astype(low)
    n2_out[...] = n2
    rotated = [chip_bits[c:] + chip_bits[:c] for c in range(3)]
    rows_two = Doubling(at, n2_out, n_all, n_sem, n_core_sem, rotated)
    rows_two.start()
    weights[1].start(1, 3)

    router_rows = jnp.concatenate([router[...], jnp.zeros((128 - exps, width), full)], axis=0)
    logits = nt(n2.astype(full), router_rows, precision=highest)
    lane = lane_of((rows, 128))
    logits = jnp.where(lane < exps, logits, -1e30)
    probs = jnp.exp(logits - jnp.max(logits, axis=1, keepdims=True))
    probs = probs / jnp.sum(probs, axis=1, keepdims=True)
    probs_out[...] = probs
    picked = jnp.where(routed(routes_t, at.me, rows), probs, 0.0)
    comb = picked / jnp.sum(picked, axis=1, keepdims=True)
    comb = jnp.where(row_of((rows, 1)) < lengths[at.me], comb, 0.0)
    comb_send[...] = comb.T[0 : comb_send.shape[0]]

    def comb_copy(k):
        other = (plane + k) % members
        return send(
            comb_send,
            comb_all.at[plane],
            comb_sem.at[SEND, other],
            comb_sem.at[RECV, plane],
            (at.grp, other // exps, other % exps),
        )

    def start_comb(k, _):
        comb_copy(k).start()
        return 0

    lax.fori_loop(1, members, start_comb, 0)
    pltpu.make_async_copy(comb_send, comb_all.at[plane], comb_sem.at[RECV, plane]).start()
    rows_two.next(0)
    weights[1].start(3, 5)

    stores = [
        (qkv, qkv_out),
        (pb, pb_out),
        (mine, mine_out),
        (n1, n1_out),
        (wqkv, wqkv_out),
        (wout, wout_out),
        (in_low, in_out),
        (down_slab, down_out),
    ]
    for i, (src, dst) in enumerate(stores):
        pltpu.make_async_copy(src, dst, store_sem.at[i]).start()

    rows_two.next(1)
    weights[1].start(5)
    for step in range(2, rows_two.steps):
        rows_two.next(step)
    for step in range(2, cots.steps):
        cots.next(step)

    cots.finish_in()
    rows_two.finish_in()

    def comb_in(k, _):
        arrived(comb_all.at[k], comb_sem.at[RECV, k])
        return 0

    lax.fori_loop(0, members, comb_in, 0)
    for tile in weights:
        tile.arrive()

    for k in range(1, exps):
        peer = exp_peer(k)
        arrived(mine.at[peer], ctx_sem.at[SEND, peer])
    over_segments(lambda copy: copy.wait_send(), lambda k, src, dst: None)
    for k in range(1, reps):
        arrived(out_w, wo_sem.at[SEND, (at.rep + k) % reps])
    group_tokens.sent()
    group_wout.sent()
    cots.finish_out()
    rows_two.finish_out()

    def sent_comb(k, _):
        comb_copy(k).wait_send()
        return 0

    lax.fori_loop(1, members, sent_comb, 0)
    for tile in weights:
        tile.sent()
    for i, (src, dst) in enumerate(stores):
        pltpu.make_async_copy(src, dst, store_sem.at[i]).wait()


def forward_call(
    grps, exps, lengths, bias_table, routes_t, tokens, cotangent, gains, router, attn_qkv, attn_out, expert_in, expert_out
):
    reps = grps * QUAD
    rows, width = tokens.shape
    head_cols = width // exps
    row_block, shard_cols = attn_qkv.shape
    seg = math.gcd(shard_cols, head_cols)
    segs = shard_cols // seg
    units = expert_out.shape[0]
    out_cols = attn_out.shape[1]
    heads = HEADS // exps
    members = QUAD * exps
    tiles = Tiles(units, reps)
    shape = jax.ShapeDtypeStruct
    vmem = pl.BlockSpec(memory_space=pltpu.VMEM)
    smem = pl.BlockSpec(memory_space=pltpu.SMEM)
    hbm = pl.BlockSpec(memory_space=pl.ANY)
    results = [
        (shape((2, width, 2 * tiles.size), low), hbm),
        (shape((2, tiles.size, width), low), hbm),
        (shape((members, rows, width), low), hbm),
        (shape((members, rows, width), low), hbm),
        (shape((members, 8, rows), full), hbm),
        (shape((exps, rows, 3 * head_cols), low), hbm),
        (shape((exps * heads, rows, rows), low), hbm),
        (shape((exps, rows, head_cols), low), hbm),
        (shape((exps, rows, width), low), hbm),
        (shape((exps, 3 * head_cols, row_block), low), hbm),
        (shape((exps, reps, row_block, out_cols), low), hbm),
        (shape((rows, width), full), vmem),
        (shape((rows, width), low), vmem),
        (shape((rows, 128), full), vmem),
        (shape(expert_in.shape, low), hbm),
        (shape(expert_out.shape, low), hbm),
    ]
    dma = pltpu.SemaphoreType.DMA
    chips = members // 2
    return pl.pallas_call(
        functools.partial(forward_kernel, grps, exps),
        out_shape=[r[0] for r in results],
        in_specs=[smem] * 2 + [vmem] * 7 + [hbm] * 2,
        out_specs=[r[1] for r in results],
        scratch_shapes=[
            pltpu.VMEM(expert_in.shape, full),
            pltpu.VMEM(expert_out.shape, full),
            pltpu.VMEM((shard_cols, row_block), low),
            pltpu.VMEM((row_block, out_cols), low),
            pltpu.VMEM(expert_in.shape, low),
            pltpu.VMEM(expert_out.shape, low),
            pltpu.VMEM((exps, rows, width), low),
            pltpu.VMEM((exps, 3 * head_cols, row_block), low),
            pltpu.VMEM((exps, reps, row_block, out_cols), low),
            pltpu.VMEM((exps, rows, width), low),
            pltpu.VMEM((exps, rows, 3 * head_cols), low),
            pltpu.VMEM((exps * heads, rows, rows), low),
            pltpu.VMEM((exps, rows, head_cols), low),
            pltpu.VMEM((exps, rows, head_cols), low),
            pltpu.VMEM((heads, rows, rows), full),
            pltpu.VMEM((8, rows), full),
            pltpu.VMEM((tiles.skip, width), low),
            dma((2, exps)),
            dma((2, max(segs * reps, exps * 3 * head_cols // seg))),
            dma((2, reps)),
            dma((2, exps)),
            dma((2, 2, 2 * reps)),
            dma((2, 2, reps + 1)),
            dma((2, exps)),
            dma((2, 3 * chips)),
            dma((2, 3 * chips + 1)),
            dma((2, 3 * chips)),
            dma((2, 3 * chips + 1)),
            dma((2, members)),
            dma((8,)),
            dma((2,)),
        ],
        compiler_params=pltpu.CompilerParams(
            collective_id=0, has_side_effects=True, vmem_limit_bytes=60 * 1024 * 1024
        ),
        name="forward",
    )(lengths, bias_table, routes_t, tokens, cotangent, gains, router, attn_qkv, attn_out, expert_in, expert_out)


def expert_kernel(
    grps,
    exps,
    cap,
    deal,
    routes_t,
    comb,
    n_all,
    cot_all,
    both_w,
    down_w,
    in_low,
    down_slab,
    h1,
    n_total,
    y_half,
    y_far,
    c_in,
    both_g,
    down_g,
    in_parts,
    down_parts,
    place,
    marks,
    n_rows,
    g_rows,
    both_v,
    down_v,
    raw_n,
    raw_g,
    y_acc,
    n_acc,
    both_d,
    active,
    n_bufs,
    c_sum,
    out_y,
    load_sem,
    raw_sem,
    out_sem,
    in_sem,
    in_down_sem,
    home_sem,
    home_down_sem,
    stage_sem,
    far_sem,
    n_sem,
    c_sem,
):
    at = Where(grps, exps)
    rows, width = n_all.shape[1:]
    tiles = Tiles(down_slab.shape[0], at.reps)
    size = tiles.size
    slots = exps * cap
    members = QUAD * exps
    loads = [pltpu.make_async_copy(both_w.at[t], both_v.at[t], load_sem.at[0, t]) for t in range(2)] + [
        pltpu.make_async_copy(down_w.at[t], down_v.at[t], load_sem.at[1, t]) for t in range(2)
    ]
    for copy in loads:
        copy.start()

    def raw_copies(q):
        here = pl.ds(pl.multiple_of(q * exps, exps), exps)
        return [
            pltpu.make_async_copy(n_all.at[here], raw_n.at[pl.ds(q % 2 * exps, exps)], raw_sem.at[0, q % 2]),
            pltpu.make_async_copy(cot_all.at[here], raw_g.at[pl.ds(q % 2 * exps, exps)], raw_sem.at[1, q % 2]),
        ]

    for copy in raw_copies(0):
        copy.start()

    beside = at.exp + 1 - 2 * (at.exp % 2)
    greet(*neighbours(at))()
    last = tiles.count - 1
    incoming = Outward(
        at, tiles, last, in_low, down_slab, both_v.at[last], down_v.at[last], None, in_sem, in_down_sem
    )
    incoming.start()
    home = Homeward(
        at, tiles, 0, both_v.at[0], down_v.at[0], in_parts, down_parts, home_sem, home_down_sem
    )

    earlier = jnp.where(row_of((rows, rows)) < lane_of((rows, rows)), 1.0, 0.0).astype(low)
    slot = row_of((cap, rows)).astype(full)

    def dispatch(q, _):
        @pl.when(q + 1 < QUAD)
        def _():
            for copy in raw_copies(q + 1):
                copy.start()

        for copy in raw_copies(q):
            copy.wait()
        lines = []
        for j in range(exps):
            seq = at.grp * members + q * exps + j
            pair = routes_t[:, pl.ds(pl.multiple_of(seq * rows, rows), rows)]
            lines.append(jnp.logical_or(pair[0:1] == at.exp, pair[1:2] == at.exp))
        lines = [jnp.where(line, 1.0, 0.0) for line in lines] + [jnp.zeros((8 - exps, rows), full)]
        hot_low = jnp.concatenate(lines, axis=0).astype(low)
        before = dot(hot_low, earlier)
        for j in range(exps):
            s = q * exps + j
            inside = jnp.logical_and(slot == before[j : j + 1, :], hot_low[j : j + 1, :].astype(full) > 0.5)
            here = jnp.where(inside, 1.0, 0.0)
            place[s] = here.astype(low)
            g = raw_g[q % 2 * exps]
            for b in range(1, exps):
                g = jnp.where(deal[at.grp * members + s] == at.grp * members + q * exps + b, raw_g[q % 2 * exps + b], g)
            where = pl.ds(pl.multiple_of(s * cap, cap), cap)
            n_rows[where] = dot(here.astype(low), raw_n[q % 2 * exps + j]).astype(low)
            g_rows[where] = dot(here.astype(low), g).astype(low)
            marks[where, 0:1] = jnp.sum(here * comb[s, pl.ds(at.exp, 1), :], axis=1, keepdims=True)
            marks[where, 1:2] = jnp.zeros((cap, 1), full)
        return 0

    lax.fori_loop(0, QUAD, dispatch, 0)
    for copy in loads:
        copy.wait()
    curve = math.sqrt(2.0 / math.pi)

    core = at.exp % 2

    plane = at.quad * exps + at.exp
    sibling = at.device(at.rep, beside)
    dn = Halving(at, n_bufs, n_sem, [[0, 1, 2], [1, 2, 0], [2, 0, 1]])

    def n_copy(j):
        return send(raw_n.at[j], n_bufs[0].at[j], far_sem.at[0, 0, j], far_sem.at[0, 1, j], sibling)

    def y_copies(j):
        return (
            pltpu.make_async_copy(out_y.at[j % 2], y_half.at[j], out_sem.at[j % 2]),
            send(raw_n.at[j], y_far.at[j], far_sem.at[1, 0, j], far_sem.at[1, 1, j], sibling),
        )

    def c_copy(k):
        other = (plane + k) % members
        return send(
            c_sum.at[other],
            c_in.at[plane],
            c_sem.at[0, other],
            c_sem.at[1, plane],
            (at.grp, other // exps, other % exps),
        )

    def slots_of(s):
        return pl.ds(pl.multiple_of(s * cap, cap), cap)

    def n_rows_of(s):
        where = slots_of(s)
        line = jnp.sum(place[s].astype(full) * marks[where, 1:2], axis=0, keepdims=True)
        c_sum[s] = jnp.broadcast_to(line, (8, rows))
        return tn(place[s], n_acc[where]).astype(low)

    def y_rows_of(p):
        first = p // exps * exps
        spot = at.grp * members + p
        here, y = place[first], y_acc[slots_of(first)]
        for c in range(1, exps):
            taken = deal[at.grp * members + first + c] == spot
            here = jnp.where(taken, place[first + c], here)
            y = jnp.where(taken, y_acc[slots_of(first + c)], y)
        return (tn(here, y) + jnp.where(deal[at.me] == spot, h1[...], 0.0)).astype(low)

    def give_n(j):
        raw_n[j] = n_rows_of(2 * j + 1 - core)
        n_copy(j).start()
        raw_g[j] = n_rows_of(2 * j + core)

    def add_n(quad):
        for k in range(exps // 2):
            j = quad * (exps // 2) + k
            arrived(n_bufs[0].at[j], far_sem.at[0, 1, j])
            n_bufs[0][j] = n_bufs[0][j] + raw_g[j]

    def give_y(j, _):
        @pl.when(j >= 2)
        def _():
            y_copies(j - 2)[0].wait()

        out_y[j % 2] = y_rows_of(2 * j + core)
        n_copy(j).wait_send()
        raw_n[j] = y_rows_of(2 * j + 1 - core)
        for copy in y_copies(j):
            copy.start()
        return 0

    def start_c(k, _):
        c_copy(k).start()
        return 0

    def tile_work(f, _):
        @pl.when(f == last)
        def _():
            incoming.arrive()

        def chunk(i, _):
            c = jnp.where(i == 0, at.near(3), jnp.where(i == 1, at.near(1), jnp.where(i == 2, at.near(2), at.quad)))
            here = pl.ds(pl.multiple_of(c * slots, slots), slots)
            share = marks[here, 0:1]
            both = dot(n_rows[here], both_v[f])
            gate_part, up_part = both[:, :size], both[:, size:]
            grad = nt(g_rows[here], down_v[f])
            square = gate_part * gate_part
            bend = jnp.tanh(curve * gate_part * (1.0 + 0.044715 * square))
            half = 0.5 * (1.0 + bend)
            gelu = gate_part * half
            slope = half + (0.5 * curve) * gate_part * (1.0 - bend * bend) * (1.0 + (3 * 0.044715) * square)
            value = gelu * up_part
            marks[here, 1:2] += jnp.sum(value * grad, axis=1, keepdims=True)
            grad = grad * share
            active[f % 2, here] = (value * share).astype(low)
            both_d[f % 2, here, :size] = (grad * up_part * slope).astype(low)
            both_d[f % 2, here, size:] = (grad * gelu).astype(low)
            y = dot(active[f % 2, here], down_v[f])
            y_acc[here] = jnp.where(f == 0, y, y_acc[here].astype(full) + y).astype(low)
            n_back = nt(both_d[f % 2, here], both_v[f])
            n_acc[here] = jnp.where(f == 0, n_back, n_acc[here].astype(full) + n_back).astype(low)

            @pl.when(f == last)
            def _():
                for k in range(exps // 2):
                    give_n(c * (exps // 2) + k)

            @pl.when(jnp.logical_and(f == last, i == 2))
            def _():
                add_n(at.near(3))

            @pl.when(jnp.logical_and(f == last, i == 3))
            def _():
                add_n(at.near(1))
                dn.start(0, 1)

            return 0

        lax.fori_loop(0, QUAD, chunk, 0)

        @pl.when(f == 0)
        def _():
            weight_work(0)
            home.start()

        return 0

    def weight_work(f):
        def columns(m, _):
            cols = pl.ds(pl.multiple_of(m * (width // 2), width // 2), width // 2)
            both_v[f, cols] = tn(n_rows[:, cols], both_d[f % 2]).astype(low)
            down_v[f, :, cols] = tn(active[f % 2], g_rows[:, cols]).astype(low)
            return 0

        lax.fori_loop(0, 2, columns, 0)

        for copy in stage_copies(f):
            copy.start()

    def stage_copies(f):
        if f == 0:
            return []
        return [
            pltpu.make_async_copy(both_v.at[f], both_g.at[f - 1], stage_sem.at[0, f]),
            pltpu.make_async_copy(down_v.at[f], down_g.at[f - 1], stage_sem.at[1, f]),
        ]

    lax.fori_loop(0, tiles.count, tile_work, 0)

    half = members // 2
    lax.fori_loop(1, members, start_c, 0)
    c_in[plane] = c_sum[plane]
    weight_work(1)
    add_n(at.near(2))
    dn.start(0, 2)
    add_n(at.quad)
    dn.start(0, 0)
    weight_work(2)
    lax.fori_loop(0, half, give_y, 0)
    for step in range(len(dn.chip_bits)):
        dn.next(step)
    n_total[...] = dn.result()[0]
    for j in (half - 2, half - 1):
        y_copies(j)[0].wait()
    for f in range(tiles.count):
        for copy in stage_copies(f):
            copy.wait()

    def core_in(j, _):
        y_copies(j)[1].wait_send()
        arrived(y_far.at[j], far_sem.at[1, 1, j])
        return 0

    lax.fori_loop(0, half, core_in, 0)

    def c_done(k, _):
        c_copy(k).wait_send()
        other = (plane + k) % members
        arrived(c_in.at[other], c_sem.at[1, other])
        return 0

    lax.fori_loop(1, members, c_done, 0)
    dn.finish()
    home.arrive()
    incoming.sent()
    home.sent()


def expert_call(grps, exps, cap, deal, routes_t, comb_all, n_all, cot_all, both_w, down_w, in_low, down_slab, h1):
    members, rows, width = n_all.shape
    reps = grps * QUAD
    tiles = Tiles(down_slab.shape[0], reps)
    size = tiles.size
    slab, both_hidden = in_low.shape
    units = down_slab.shape[0]
    slots = exps * cap
    chip_bits = bits_of(members) - 1
    shape = jax.ShapeDtypeStruct
    vmem = pl.BlockSpec(memory_space=pltpu.VMEM)
    smem = pl.BlockSpec(memory_space=pltpu.SMEM)
    hbm = pl.BlockSpec(memory_space=pl.ANY)
    results = [
        (shape((rows, width), low), vmem),
        (shape((members // 2, rows, width), low), hbm),
        (shape((members // 2, rows, width), low), hbm),
        (shape((members, 8, rows), full), vmem),
        (shape((2, width, 2 * size), low), hbm),
        (shape((2, size, width), low), hbm),
        (shape((grps, slab, both_hidden), low), hbm),
        (shape((grps, units, width), low), hbm),
    ]
    dma = pltpu.SemaphoreType.DMA
    return pl.pallas_call(
        functools.partial(expert_kernel, grps, exps, cap),
        out_shape=[r[0] for r in results],
        in_specs=[smem] + [vmem] * 2 + [hbm] * 6 + [vmem],
        out_specs=[r[1] for r in results],
        scratch_shapes=[
            pltpu.VMEM((members, cap, rows), low),
            pltpu.VMEM((QUAD * slots, 128), full),
            pltpu.VMEM((QUAD * slots, width), low),
            pltpu.VMEM((QUAD * slots, width), low),
            pltpu.VMEM((tiles.count, width, 2 * size), low),
            pltpu.VMEM((tiles.count, size, width), low),
            pltpu.VMEM((2 * exps, rows, width), low),
            pltpu.VMEM((2 * exps, rows, width), low),
            pltpu.VMEM((QUAD * slots, width), low),
            pltpu.VMEM((QUAD * slots, width), low),
            pltpu.VMEM((2, QUAD * slots, 2 * size), low),
            pltpu.VMEM((2, QUAD * slots, size), low),
            [pltpu.VMEM((members >> (1 + step), rows, width), low) for step in range(chip_bits + 1)],
            pltpu.VMEM((members, 8, rows), full),
            pltpu.VMEM((2, rows, width), low),
            dma((2, 2)),
            dma((2, 2)),
            dma((2,)),
            dma((2, 2 * reps)),
            dma((2, reps + 1)),
            dma((2, 2 * reps)),
            dma((2, max(QUAD, grps))),
            dma((2, tiles.count)),
            dma((2, 2, members // 2)),
            dma((2, 3 << chip_bits)),
            dma((2, members)),
        ],
        compiler_params=pltpu.CompilerParams(
            collective_id=2, has_side_effects=True, vmem_limit_bytes=60 * 1024 * 1024
        ),
        name="experts",
    )(deal, routes_t, comb_all, n_all, cot_all, both_w, down_w, in_low, down_slab, h1)


def adamw_root(weight, moment, second, gradient, step_rate, decay_factor):
    new_moment = beta_one * moment + (1.0 - beta_one) * gradient
    new_second = beta_two * second + (1.0 - beta_two) * gradient * gradient
    root = lax.rsqrt(new_second * (1.0 / (1.0 - beta_two**STEP)))
    step = new_moment * (root * (1.0 - eps_adam * root))
    keep = 1.0 - step_rate * decay_factor
    return (new_moment, new_second, keep * weight - (step_rate / (1.0 - beta_one**STEP)) * step)


def adam_kernel(exps, *refs):
    in_parts, down_parts, qkv_grad, out_grad, small = refs[:5]
    states, news, bias_grad = refs[5:26], refs[26:47], refs[47]
    heads = HEADS // exps
    width = small.shape[1]

    def update(i, grad, rate, decay):
        weight, first, second = [state[...] for state in states[3 * i : 3 * i + 3]]
        values = adamw_root(weight, first, second, grad, rate, decay)
        for new, value in zip(news[3 * i : 3 * i + 3], values, strict=True):
            new[...] = value

    def total(parts):
        result = parts[0].astype(full)
        for k in range(1, parts.shape[0]):
            result = result + parts[k].astype(full)
        return result

    @pl.when(pl.program_id(0) == 0)
    def _():
        update(0, qkv_grad[...], 1.5 / math.sqrt(D), 0.1)
        update(1, out_grad[...], 6.0 / math.sqrt(D), 0.1)
        for e in range(exps):
            for h in range(heads):
                bias_grad[e * heads + h : e * heads + h + 1, :] = small[
                    exps + 3 + e : exps + 4 + e, h * 128 : h * 128 + BUCKETS
                ]
        update(2, bias_grad[...], 0.3, 0.0)
        update(3, small[0:exps, :], 1.0 / math.sqrt(D), 0.1)
        update(4, small[exps : exps + 2, :], 0.5, 0.0)

    update(5, total(in_parts), 1.5 / math.sqrt(D), 0.1)
    update(6, total(down_parts), 1.5 / math.sqrt(FF), 0.1)


def adam_call(exps, in_parts, down_parts, qkv_grad, out_grad, small, states):
    steps = 4

    def whole(array):
        return pl.BlockSpec(array.shape, lambda i: (0,) * array.ndim)

    def columns(array):
        block = array.shape[:-1] + (array.shape[-1] // steps,)
        return pl.BlockSpec(block, lambda i: (0,) * (array.ndim - 1) + (i,))

    specs = [whole(state) for state in states[:15]]
    specs += [columns(state) for state in states[15:18]] + [columns(state) for state in states[18:]]
    return pl.pallas_call(
        functools.partial(adam_kernel, exps),
        grid=(steps,),
        in_specs=[columns(in_parts), columns(down_parts), whole(qkv_grad), whole(out_grad), whole(small)] + specs,
        out_specs=specs,
        out_shape=[jax.ShapeDtypeStruct(state.shape, full) for state in states],
        scratch_shapes=[pltpu.VMEM((HEADS, BUCKETS), full)],
        compiler_params=pltpu.CompilerParams(vmem_limit_bytes=60 * 1024 * 1024),
        name="adam",
    )(in_parts, down_parts, qkv_grad, out_grad, small, *states)


def backward_kernel(
    grps,
    exps,
    lengths,
    deal,
    y_half,
    y_far,
    both_g,
    down_g,
    in_before,
    down_before,
    n1_in,
    cot_all,
    routes_t,
    tokens,
    n_total,
    c_in,
    n2_in,
    probs_in,
    h1_from,
    qkv_from,
    pb_from,
    mine_from,
    wqkv_from,
    wout_from,
    gains,
    router_t,
    *rest,
):
    token_grad, block_out, in_parts, down_parts, qkv_grad, out_grad, small_out = rest[:7]
    scratch = rest[7:]
    (
    h1_in,
    qkv,
    pb,
    mine,
    wqkv,
    wout,
    kept,
    y_bufs,
    dh1,
    dz_send,
    dz_all,
    do_send,
    do_in,
    bias_sum,
    dqkv,
    dqkv_t,
    dn1_send,
    dn1_in,
    wq_send,
    og_send,
    mids,
    far_send,
    far_in,
    small_send,
    small_exp,
    small_sum,
    small_rep,
    small_half,
    small_far,
    y_sem,
    load_sem,
    weight_sem,
    down_sem,
    dz_sem,
    do_sem,
    dn1_sem,
    wq_sem,
    og_sem,
    mid_sem,
    far_sem,
    small_sem,
    small2_sem,
    small3_sem,
    n1_sem,
    operand_sem,
    ) = scratch
    at = Where(grps, exps)
    reps = at.reps
    rows, width = tokens.shape
    heads = HEADS // exps
    head_dim = width // HEADS
    head_cols = heads * head_dim
    block_cols = min(128, head_cols)
    row_block = wqkv.shape[2]
    out_cols = wout.shape[3]
    tiles = Tiles(down_parts.shape[1], reps)
    scale = 1.0 / math.sqrt(head_dim)
    SEND, RECV = 0, 1
    plane = at.quad * exps + at.exp
    members = QUAD * exps

    def exp_peer(k):
        return (at.exp + k) % exps

    router = router_t[...]
    met = greet(*neighbours(at))
    n1 = kept.at[0:exps]
    group = pl.ds(pl.multiple_of(at.quad * exps, exps), exps)
    cot_copy = pltpu.make_async_copy(cot_all.at[group], dn1_send, n1_sem.at[1])
    cot_copy.start()
    loads = [
        pltpu.make_async_copy(src, dst, operand_sem.at[i])
        for i, (src, dst) in enumerate(
            ((h1_from, h1_in), (wout_from, wout), (qkv_from, qkv), (pb_from, pb), (mine_from, mine), (wqkv_from, wqkv))
        )
    ]
    ys = Halving(at, y_bufs, y_sem, [[0, 1, 2], [1, 2, 0], [2, 0, 1]])
    half_loads = [
        pltpu.make_async_copy(y_far, y_bufs[0], load_sem.at[0]),
        pltpu.make_async_copy(y_half, kept, load_sem.at[1]),
    ]
    for copy in loads + half_loads:
        copy.start()

    span = 2 * rows
    met()

    homes = [
        Homeward(
            at, tiles, t + 1, both_g.at[t], down_g.at[t], in_parts, down_parts, weight_sem.at[t], down_sem.at[t]
        )
        for t in range(2)
    ]
    homes[0].start()
    n1_copy = pltpu.make_async_copy(n1_in, n1, n1_sem.at[0])

    lane = lane_of((rows, 128))
    comb_rows = []
    for e in range(exps):
        total = c_in[e]
        for q in range(1, QUAD):
            total = total + c_in[q * exps + e]
        comb_rows.append(total[0:1, :])
    comb_rows.append(jnp.zeros((128 - exps, rows), full))
    comb_grad = jnp.concatenate(comb_rows, axis=0).T
    valid = row_of((rows, 1)) < lengths[at.me]
    probs = probs_in[...]
    hot = routed(routes_t, at.me, rows)
    picked = jnp.where(hot, probs, 0.0)
    total = jnp.sum(picked, axis=1, keepdims=True)
    gate = picked / total
    gate_grad_rows = jnp.where(valid, comb_grad, 0.0)
    spread_grad = jnp.sum(gate_grad_rows * gate, axis=1, keepdims=True)
    probs_grad = jnp.where(hot, (gate_grad_rows - spread_grad) / total, 0.0)
    logit_grad = probs * (probs_grad - jnp.sum(probs_grad * probs, axis=1, keepdims=True))
    small_rows = small_send.shape[0]
    small_send[...] = jnp.zeros_like(small_send)
    router_back = jnp.dot(
        logit_grad, jnp.concatenate([router, jnp.zeros((128 - exps, width), full)], axis=0),
        precision=highest, preferred_element_type=full,
    )
    for copy in loads:
        copy.wait()
    h1 = h1_in[...]
    r2 = lax.rsqrt(jnp.mean(h1 * h1, axis=1, keepdims=True) + eps_norm)

    steps = len(ys.chip_bits)
    n2_grad = router_back + n_total[...].astype(full)
    scaled = n2_grad * gains[1:2, :]
    cot_copy.wait()
    dealt = deal[at.me] - at.base
    g = dn1_send[0]
    for e in range(1, exps):
        g = jnp.where(dealt == e, dn1_send[e], g)
    hidden_grad = (
        jnp.where(valid, g.astype(full), 0.0)
        + r2 * scaled
        - h1 * (r2 * r2 * r2) * jnp.mean(scaled * h1, axis=1, keepdims=True)
    )
    dh1[...] = hidden_grad
    small_send[exps + 1 : exps + 2, :] = jnp.sum(n2_grad * h1 * r2, axis=0, keepdims=True)
    branch = hidden_grad.astype(low)
    dz_send[...] = branch
    for e in range(exps):
        total = jnp.zeros((rows, row_block), full)
        for r in range(reps):
            total = total + nt(branch[:, r * out_cols : (r + 1) * out_cols], wout[e, r])
        do_send[e] = total.astype(low)

    def do_copies():
        return [
            send(
                do_send.at[exp_peer(k)],
                do_in.at[at.exp],
                do_sem.at[SEND, exp_peer(k)],
                do_sem.at[RECV, at.exp],
                at.device(at.rep, exp_peer(k)),
            )
            for k in range(1, exps)
        ]

    for copy in do_copies():
        copy.start()
    pltpu.make_async_copy(do_send.at[at.exp], do_in.at[at.exp], do_sem.at[RECV, at.exp]).start()

    group_dz = Group(at, dz_send, dz_all, dz_sem)
    dz_all[at.exp] = branch
    for copy in half_loads:
        copy.wait()

    def add_halves(j, _):
        y_bufs[0][j] = y_bufs[0][j] + kept[j]
        return 0

    lax.fori_loop(0, kept.shape[0], add_halves, 0)
    n1_copy.start()

    bias_sum[...] = jnp.zeros_like(bias_sum)

    def dn1_copies():
        beside, across = turn(at.exp, 2), turn(at.exp, 1)
        return [
            functools.partial(
                send, dn1_send.at[k], dn1_in.at[j], dn1_sem.at[SEND, j], dn1_sem.at[RECV, j], at.device(at.rep, to)
            )
            for k, j, to in ((turn(at.exp, 0), 2, beside), (across, 0, across), (beside, 1, beside))
        ]

    def attend_back(i, _):
        s = turn(at.exp, i)
        arrived(do_in.at[s], do_sem.at[RECV, s])

        @pl.when(i == 0)
        def _():
            group_dz.start()
            ys.start(0)

        @pl.when(i == 2)
        def _():
            group_dz.pass_on()

        block_lane = lane_of((rows, block_cols))
        for c in range(head_cols // block_cols):
            cols = slice(c * block_cols, (c + 1) * block_cols)
            k_cols = slice(head_cols + c * block_cols, head_cols + (c + 1) * block_cols)
            v_cols = slice(2 * head_cols + c * block_cols, 2 * head_cols + (c + 1) * block_cols)
            q = qkv[s, :, cols] * scale
            k = qkv[s, :, k_cols]
            v = qkv[s, :, v_cols]
            do = do_in[s, :, cols]
            dq = jnp.zeros((rows, block_cols), full)
            dk = jnp.zeros((rows, block_cols), full)
            dv = jnp.zeros((rows, block_cols), full)
            for t in range(block_cols // head_dim):
                h = c * (block_cols // head_dim) + t
                here = jnp.logical_and(block_lane >= t * head_dim, block_lane < (t + 1) * head_dim)
                zero = jnp.zeros_like(q)
                do_h = jnp.where(here, do, zero)
                weights = pb[s * heads + h]
                p = weights.astype(full)
                dp = nt(do_h, v)
                delta = jnp.sum(dp * p, axis=1, keepdims=True)
                ds = (p * (dp - delta)).astype(low)
                bias_sum[h] += ds.astype(full)
                dv = jnp.where(here, tn(weights, do), dv)
                dq = jnp.where(here, jnp.dot(ds, k, preferred_element_type=full), dq)
                dk = jnp.where(here, tn(ds, q), dk)
            dqkv[:, cols] = (dq * scale).astype(low)
            dqkv[:, k_cols] = dk.astype(low)
            dqkv[:, v_cols] = dv.astype(low)
        dqkv_t[:, pl.ds(pl.multiple_of(s * rows, rows), rows)] = dqkv[...].T
        for e in range(exps):
            dn1_send[s, :, e * row_block : (e + 1) * row_block] = jnp.dot(
                dqkv[...], wqkv[e], preferred_element_type=full
            ).astype(low)

        @pl.when(i == 0)
        def _():
            dn1_copies()[0]().start()

        @pl.when(i == 1)
        def _():
            arrived(dn1_in.at[2], dn1_sem.at[RECV, 2])
            dn1_send[s] = (dn1_send[s].astype(full) + dn1_in[2].astype(full)).astype(low)
            dn1_copies()[1]().start()

        @pl.when(i == 2)
        def _():
            dn1_copies()[2]().start()

        return 0

    lax.fori_loop(0, exps, attend_back, 0)

    n1_copy.wait()
    seg = wq_send.shape[2]
    parts = wq_send.shape[1]
    segs = mids.shape[1] - 1
    for e in range(exps):
        part = kept[0:exps, :, e * row_block : (e + 1) * row_block].reshape(exps * rows, row_block)
        total = dot(dqkv_t[...], part)
        for j in range(parts):
            wq_send[e, j] = total[j * seg : (j + 1) * seg].astype(low)

    def owner(j):
        section, within = j // (head_cols // seg), j % (head_cols // seg)
        col = section * width + at.exp * head_cols + within * seg
        block = col // seg
        return block // segs, block % segs

    def mid_place(grp, k, quad):
        return (grp * (segs + 1) + k) * QUAD + quad

    def mid_copy(src, send_sem, rep, k, e):
        dst = mids.at[rep // QUAD, k, at.quad]
        recv = mid_sem.at[mid_place(rep // QUAD, k, at.quad)]
        stays = jnp.logical_and(rep % QUAD == at.quad, e == at.exp)
        return (
            stays,
            functools.partial(send, src, dst, send_sem, recv, (at.grp, rep % QUAD, e)),
            functools.partial(pltpu.make_async_copy, src, dst, recv),
        )

    def wq_copy(i):
        e, j = i // parts, i % parts
        rep, k = owner(j)
        return mid_copy(wq_send.at[e, j], wq_sem.at[i], rep, k, e)

    def og_copy(r):
        return mid_copy(og_send.at[r], og_sem.at[r], r, segs, at.exp)

    def go(copies, act, act_local):
        stays, away, local = copies

        @pl.when(jnp.logical_not(stays))
        def _():
            act(away)

        if act_local:

            @pl.when(stays)
            def _():
                act_local(local)

    def over(count, copies, act, act_local):
        def one(i, _):
            go(copies(i), act, act_local)
            return 0

        lax.fori_loop(0, count, one, 0)

    over(exps * parts, wq_copy, lambda copy: copy().start(), lambda copy: copy().start())
    group_dz.arrive()
    grad = tn(mine[...].reshape(exps * rows, head_cols), dz_all[...].reshape(exps * rows, width))
    for r in range(reps):
        og_send[r] = grad[:, r * out_cols : (r + 1) * out_cols].T.astype(low)
    over(reps, og_copy, lambda copy: copy().start(), lambda copy: copy().start())
    ys.next(0)
    homes[1].start()

    n1_grad = dn1_send[at.exp].astype(full)
    for j in range(2):
        arrived(dn1_in.at[j], dn1_sem.at[RECV, j])
        n1_grad = n1_grad + dn1_in[j].astype(full)
    x = tokens[...].astype(full)
    r1 = lax.rsqrt(jnp.mean(x * x, axis=1, keepdims=True) + eps_norm)
    scaled = n1_grad * gains[0:1, :]
    token_grad[...] = (
        dh1[...] + r1 * scaled - x * (r1 * r1 * r1) * jnp.mean(scaled * x, axis=1, keepdims=True)
    )
    small_send[exps : exps + 1, :] = jnp.sum(n1_grad * x * r1, axis=0, keepdims=True)

    ys.next(1)
    router_rows = lax.dot_general(
        logit_grad, n2_in[...].astype(full), (((0,), (0,)), ((), ())), preferred_element_type=full, precision=highest
    )
    small_send[0:exps, :] = router_rows[0:exps, :]

    flip = jnp.where(row_of((rows, rows)) + lane_of((rows, rows)) == rows - 1, 1.0, 0.0).astype(low)
    diagonals = []
    for h in range(heads):
        high = bias_sum[h].astype(low)
        rest = (bias_sum[h] - high.astype(full)).astype(low)
        flipped = dot(high, flip) + dot(rest, flip)
        square = jnp.concatenate([flipped, jnp.zeros((rows, rows), full)], axis=1)
        turned = pltpu.roll(square, 0, 1, stride=1, stride_axis=0)
        diagonals.append(jnp.sum(turned, axis=0, keepdims=True))
    diagonals = jnp.concatenate(diagonals + [jnp.zeros((8 - heads, span), full)], axis=0)
    in_bucket = jnp.where(bucket_of(rows - 1 - row_of((span, 128))) == lane_of((span, 128)), 1.0, 0.0)
    bias_line = jnp.dot(diagonals, in_bucket, precision=highest, preferred_element_type=full)
    for h in range(heads):
        small_send[exps + 2 : exps + 3, h * 128 : (h + 1) * 128] = bias_line[h : h + 1, :]

    def small_copies():
        return [
            send(
                small_send,
                small_exp.at[at.exp],
                small_sem.at[SEND, exp_peer(k)],
                small_sem.at[RECV, at.exp],
                at.device(at.rep, exp_peer(k)),
            )
            for k in range(1, exps)
        ]

    for copy in small_copies():
        copy.start()
    small_exp[at.exp] = small_send[...]

    def mid_sum(grp, k):
        for q in range(QUAD):
            arrived(mids.at[grp, k, q], mid_sem.at[mid_place(grp, k, q)])
        total = mids[grp, k, 0].astype(full)
        for q in range(1, QUAD):
            total = total + mids[grp, k, q].astype(full)
        return total

    far = 1 - at.grp
    for k in range(segs + 1):
        far_send[k] = mid_sum(far, k).astype(low)

    def far_copy():
        return send(far_send, far_in, far_sem.at[SEND], far_sem.at[RECV], (far, at.quad, at.exp))

    far_copy().start()
    for k in range(1, exps):
        arrived(small_exp.at[exp_peer(k)], small_sem.at[RECV, exp_peer(k)])
    total = small_exp[0]
    for e in range(1, exps):
        total = total + small_exp[e]
    small_sum[...] = total
    for e in range(exps):
        small_sum[exps + 3 + e : exps + 4 + e, :] = small_exp[e, exps + 2 : exps + 3, :]

    def small2_copies():
        return [
            send(
                small_sum,
                small_rep.at[at.quad],
                small2_sem.at[SEND, k - 1],
                small2_sem.at[RECV, at.quad],
                (at.grp, (at.quad + k) % QUAD, at.exp),
            )
            for k in range(1, QUAD)
        ]

    def small3_copy():
        return send(small_half, small_far, small3_sem.at[SEND], small3_sem.at[RECV], (far, at.quad, at.exp))

    for copy in small2_copies():
        copy.start()
    small_rep[at.quad] = small_sum[...]
    for step in range(2, steps):
        ys.next(step)
    length = lengths[at.base]
    for e in range(1, exps):
        length = jnp.where(deal[at.base + e] == at.me, lengths[at.base + e], length)
    block = ys.result()[0]
    block_out[...] = jnp.where(row_of((rows, 1)) < length, block, jnp.zeros_like(block))
    for k in range(1, QUAD):
        arrived(small_rep.at[(at.quad + k) % QUAD], small2_sem.at[RECV, (at.quad + k) % QUAD])
    total = small_rep[0]
    for q in range(1, QUAD):
        total = total + small_rep[q]
    small_half[...] = total
    small3_copy().start()
    arrived(small_far, small3_sem.at[RECV])
    total = small_half[...] + small_far[...]
    small_out[...] = total

    near = [mid_sum(at.grp, k) for k in range(segs + 1)]
    arrived(far_in, far_sem.at[RECV])
    grads = [(near[k] + far_in[k].astype(full)).T for k in range(segs + 1)]
    qkv_grad[...] = jnp.concatenate(grads[:segs], axis=1)
    out_grad[...] = grads[segs]
    for home in homes:
        home.arrive()

    ys.finish()

    for home in homes:
        home.sent()

    over(exps * parts, wq_copy, lambda copy: copy().wait_send(), None)
    over(reps, og_copy, lambda copy: copy().wait_send(), None)
    far_copy().wait_send()
    small3_copy().wait_send()
    for copies in (do_copies(), small_copies(), small2_copies()):
        for copy in copies:
            copy.wait_send()
    for copy in dn1_copies():
        copy().wait_send()
    group_dz.sent()


def routed(routes_t, seq, rows):
    pair = routes_t[:, pl.ds(pl.multiple_of(seq * rows, rows), rows)].astype(full)
    cols = jnp.concatenate([pair, jnp.zeros((126, rows), full)], axis=0).T
    lane = lane_of((rows, 128)).astype(full)
    return jnp.logical_or(lane == cols[:, 0:1], lane == cols[:, 1:2])


def backward_call(
    grps, exps, lengths, deal, y_half, y_far, both_g, down_g, in_before, down_before, n1,
    cot_all, routes_t, tokens, n_total, c_in, n2, probs, h1, qkv, pb, mine, wqkv, wout, gains, router
):
    reps = grps * QUAD
    rows, width = tokens.shape
    heads = HEADS // exps
    head_cols = width // exps
    row_block = wqkv.shape[2]
    out_cols = wout.shape[3]
    shard_cols = 3 * width // reps
    seg = math.gcd(shard_cols, head_cols)
    segs = shard_cols // seg
    parts = 3 * head_cols // seg
    members = QUAD * exps
    chip_bits = bits_of(members) - 1
    small_rows = -(-(2 * exps + 3) // 8) * 8
    shape = jax.ShapeDtypeStruct
    vmem = pl.BlockSpec(memory_space=pltpu.VMEM)
    smem = pl.BlockSpec(memory_space=pltpu.SMEM)
    hbm = pl.BlockSpec(memory_space=pl.ANY)
    results = [
        (shape((rows, width), full), vmem),
        (shape((rows, width), low), vmem),
        (shape(in_before.shape, low), hbm),
        (shape(down_before.shape, low), hbm),
        (shape((row_block, shard_cols), full), vmem),
        (shape((row_block, out_cols), full), vmem),
        (shape((small_rows, width), full), vmem),
    ]
    dma = pltpu.SemaphoreType.DMA
    bufs = [pltpu.VMEM((1 << (chip_bits - s), rows, width), low) for s in range(chip_bits + 1)]
    return pl.pallas_call(
        functools.partial(backward_kernel, grps, exps),
        out_shape=[r[0] for r in results],
        in_specs=[smem] * 2 + [hbm] * 8 + [vmem] * 6 + [hbm] * 6 + [vmem] * 2,
        out_specs=[r[1] for r in results],
        scratch_shapes=[
            pltpu.VMEM(h1.shape, full),
            pltpu.VMEM(qkv.shape, low),
            pltpu.VMEM(pb.shape, low),
            pltpu.VMEM(mine.shape, low),
            pltpu.VMEM(wqkv.shape, low),
            pltpu.VMEM(wout.shape, low),
            pltpu.VMEM((members // 2, rows, width), low),
            list(bufs),
            pltpu.VMEM((rows, width), full),
            pltpu.VMEM((rows, width), low),
            pltpu.VMEM((exps, rows, width), low),
            pltpu.VMEM((exps, rows, head_cols), low),
            pltpu.VMEM((exps, rows, head_cols), low),
            pltpu.VMEM((heads, rows, rows), full),
            pltpu.VMEM((rows, 3 * head_cols), low),
            pltpu.VMEM((3 * head_cols, exps * rows), low),
            pltpu.VMEM((exps, rows, width), low),
            pltpu.VMEM((3, rows, width), low),
            pltpu.VMEM((exps, parts, seg, row_block), low),
            pltpu.VMEM((reps, seg, row_block), low),
            pltpu.VMEM((grps, segs + 1, QUAD, seg, row_block), low),
            pltpu.VMEM((segs + 1, seg, row_block), low),
            pltpu.VMEM((segs + 1, seg, row_block), low),
            pltpu.VMEM((small_rows, width), full),
            pltpu.VMEM((exps, small_rows, width), full),
            pltpu.VMEM((small_rows, width), full),
            pltpu.VMEM((QUAD, small_rows, width), full),
            pltpu.VMEM((small_rows, width), full),
            pltpu.VMEM((small_rows, width), full),
            dma((2, 3 << chip_bits)),
            dma((2,)),
            dma((2, 2, 2 * reps)),
            dma((2, 2, max(QUAD, grps))),
            dma((2, exps)),
            dma((2, exps)),
            dma((2, exps)),
            dma((exps * parts,)),
            dma((reps,)),
            dma((grps * (segs + 1) * QUAD,)),
            dma((2,)),
            dma((2, exps)),
            dma((2, QUAD)),
            dma((2,)),
            dma((2,)),
            dma((6,)),
        ],
        compiler_params=pltpu.CompilerParams(
            collective_id=1, has_side_effects=True, vmem_limit_bytes=60 * 1024 * 1024
        ),
        input_output_aliases={6: 2, 7: 3},
        name="backward",
    )(
        lengths, deal, y_half, y_far, both_g, down_g, in_before, down_before, n1, cot_all,
        routes_t, tokens, n_total, c_in, n2, probs, h1, qkv, pb, mine, wqkv, wout, gains, router
    )


def per_device(
    tokens,
    cotangent,
    seq_lengths,
    deal,
    routes,
    attn_qkv,
    qkv_first,
    qkv_second,
    attn_out,
    out_first,
    out_second,
    rel_bias,
    bias_first,
    bias_second,
    router,
    router_first,
    router_second,
    norm_gains,
    gains_first,
    gains_second,
    expert_in,
    in_first,
    in_second,
    expert_out,
    down_first,
    down_second,
):
    rows, width = tokens.shape
    experts = router.shape[1]
    capacity = (10 * rows + 4 * experts - 1) // (4 * experts)
    exps = lax.axis_size("exp")
    grps = lax.axis_size("grp")
    routes_t = routes.T
    bias_table = rel_bias.T
    (
        both_w, down_w, cot_all, n_all, comb_all, qkv, pb, context_mine, normed_group, wqkv, wout, hidden_one,
        normed_two, router_probs, in_low, down_low,
    ) = forward_call(
        grps, exps, seq_lengths, bias_table, routes_t, tokens, cotangent, norm_gains.T, router.T,
        attn_qkv, attn_out, expert_in[0], expert_out[0],
    )
    n_total, y_half, y_far, c_in, both_g, down_g, in_before, down_before = expert_call(
        grps, exps, capacity, deal, routes_t, comb_all, n_all, cot_all, both_w, down_w, in_low, down_low,
        hidden_one,
    )
    token_grad, block_out, in_parts, down_parts, qkv_grad, out_grad, small = backward_call(
        grps, exps, seq_lengths, deal, y_half, y_far, both_g, down_g,
        in_before, down_before, normed_group, cot_all, routes_t, tokens, n_total, c_in, normed_two, router_probs, hidden_one, qkv, pb, context_mine, wqkv,
        wout, norm_gains.T, router.T,
    )
    states = [
        attn_qkv, qkv_first, qkv_second, attn_out, out_first, out_second, bias_table, bias_first.T, bias_second.T,
        router.T, router_first.T, router_second.T, norm_gains.T, gains_first.T, gains_second.T,
        expert_in[0], in_first[0], in_second[0], expert_out[0], down_first[0], down_second[0],
    ]
    new = list(adam_call(exps, in_parts, down_parts, qkv_grad, out_grad, small, states))
    new = new[:6] + [array.T for array in new[6:15]] + [array[None] for array in new[15:]]
    return (block_out, token_grad, *new)


def bucket_onehot(length):
    places = jnp.arange(length, dtype=jnp.int32)
    offset = places[None, :] - places[:, None]
    distance = jnp.abs(offset)
    bucket = 16 * (offset > 0).astype(jnp.int32)
    for threshold in thresholds:
        bucket = bucket + (distance >= threshold).astype(jnp.int32)
    return (bucket[:, :, None] == jnp.arange(BUCKETS, dtype=jnp.int32)[None, None, :]).astype(full)


def swap(pieces, axes):
    return lax.all_to_all(pieces, axes, split_axis=0, concat_axis=0, tiled=True)


def spread(block, axes):
    members = lax.axis_size(axes)
    return swap(jnp.broadcast_to(block[None], (members,) + block.shape), axes)


def plain_device(
    tokens,
    cotangent,
    seq_lengths,
    deal,
    routes,
    attn_qkv,
    qkv_first,
    qkv_second,
    attn_out,
    out_first,
    out_second,
    rel_bias,
    bias_first,
    bias_second,
    router,
    router_first,
    router_second,
    norm_gains,
    gains_first,
    gains_second,
    expert_in,
    in_first,
    in_second,
    expert_out,
    down_first,
    down_second,
):
    rows, width = tokens.shape
    head_dim = width // HEADS
    score_scale = 1.0 / math.sqrt(head_dim)
    experts = router.shape[1]
    capacity = (10 * rows + 4 * experts - 1) // (4 * experts)
    exps = lax.axis_size("exp")
    grps = lax.axis_size("grp")
    reps = grps * QUAD
    heads = HEADS // exps
    head_cols = heads * head_dim
    place = lax.axis_index("exp")
    base = lax.axis_index(REP) * exps
    me = base + place
    slab = expert_in.shape[1]
    units = expert_out.shape[1]
    quarter = grps * units

    row_block = attn_qkv.shape[0]
    qkv_rows = lax.all_gather(attn_qkv.astype(low), REP, axis=1, tiled=True)
    out_rows = lax.all_gather(attn_out.astype(low), REP, axis=1, tiled=True)
    qkv_pieces = jnp.transpose(
        qkv_rows.reshape(row_block, 3, exps, head_cols), (2, 0, 1, 3)
    ).reshape(exps, row_block, 3 * head_cols)
    qkv_mine = swap(qkv_pieces, "exp").reshape(width, 3 * head_cols)
    full_out = spread(out_rows, "exp").reshape(width, width)

    group_tokens = spread(tokens, "exp")
    group_cotangent = spread(cotangent, "exp")
    my_cotangent = lax.dynamic_index_in_dim(group_cotangent, deal[me] - base, 0, keepdims=False)

    my_routes = lax.dynamic_slice_in_dim(routes, me * rows, rows, 0)
    places = jnp.arange(rows, dtype=jnp.int32)
    valid_rows = (places < seq_lengths[me]).astype(full)
    group_lengths = lax.dynamic_slice_in_dim(seq_lengths, base, exps, 0)
    key_ok = places[None, :] < group_lengths[:, None]
    gain_one = norm_gains[:, 0]
    gain_two = norm_gains[:, 1]

    chosen = (my_routes[:, :, None] == jnp.arange(experts, dtype=jnp.int32)[None, None, :]).astype(full)
    flat_routes = my_routes.reshape(-1)
    route_hot = (flat_routes[:, None] == jnp.arange(experts, dtype=jnp.int32)[None, :]).astype(jnp.int32)
    before = jnp.cumsum(route_hot, axis=0) - route_hot
    slot_index = jnp.sum(before * route_hot, axis=-1)
    target = (flat_routes * capacity + slot_index).reshape(rows, 2)
    slots = experts * capacity
    slot_ids = jnp.arange(slots, dtype=jnp.int32)
    place_first = slot_ids[:, None] == target[None, :, 0]
    place_second = slot_ids[:, None] == target[None, :, 1]
    place_any = jnp.logical_or(place_first, place_second).astype(low)

    shard_in = expert_in[0].astype(low).reshape(slab, 2, grps, QUAD, units)
    in_pieces = jnp.transpose(shard_in, (1, 3, 0, 2, 4)).reshape(2, 1, QUAD, slab, quarter)
    in_pieces = jnp.broadcast_to(in_pieces, (2, grps, QUAD, slab, quarter)).reshape(
        2, reps, slab, quarter
    )
    down_mine = spread(expert_out[0].astype(low), "grp").reshape(quarter, width)
    gate_mine = swap(in_pieces[0], REP).reshape(width, quarter)
    up_mine = swap(in_pieces[1], REP).reshape(width, quarter)

    upstream = my_cotangent.astype(full) * valid_rows[:, None]

    def to_experts(block):
        sent = block.reshape((1, experts) + block.shape[1:])
        sent = jnp.broadcast_to(sent, (QUAD,) + sent.shape[1:])
        return swap(sent.reshape((QUAD * experts,) + block.shape[1:]), PLANE)

    def dispatch(values):
        return dot(place_any, values).astype(low).reshape(experts, capacity, width)

    expert_upstream = to_experts(dispatch(upstream.astype(low))).reshape(-1, width)
    active_grad_bare = lax.dot_general(
        expert_upstream, down_mine, (((1,), (1,)), ((), ())), preferred_element_type=full
    )

    x_group = group_tokens.astype(full)
    scale_group = lax.rsqrt(jnp.mean(x_group * x_group, axis=-1, keepdims=True) + eps_norm)
    normed_group = (x_group * scale_group * gain_one).astype(low).reshape(exps * rows, width)
    qkv = dot(normed_group, qkv_mine).astype(low).reshape(exps, rows, 3, heads, head_dim)
    queries = qkv[:, :, 0]
    key_rows = qkv[:, :, 1]
    values = qkv[:, :, 2]
    onehot = bucket_onehot(rows)
    bias_mine = lax.dynamic_slice_in_dim(rel_bias, place * heads, heads, 1)
    bias_table = jnp.einsum("ijb,bh->hij", onehot, bias_mine, precision=highest)

    def scores_of():
        raw = (
            jnp.einsum("sihd,sjhd->shij", queries, key_rows, preferred_element_type=full)
            * score_scale
            + bias_table[None]
        )
        return jnp.where(key_ok[:, None, None, :], raw, -1e30)

    scores = scores_of()
    row_max = jnp.max(scores, axis=-1, keepdims=True)
    log_total = row_max + jnp.log(jnp.sum(jnp.exp(scores - row_max), axis=-1, keepdims=True))
    weights_low = jnp.exp(scores - log_total).astype(low)
    context_mine = (
        jnp.einsum("shij,sjhd->sihd", weights_low, values, preferred_element_type=full)
        .astype(low)
        .reshape(exps, rows, head_cols)
    )
    context = jnp.transpose(swap(context_mine, "exp"), (1, 0, 2)).reshape(rows, width)

    x_float = tokens.astype(full)
    scale_one = lax.rsqrt(jnp.mean(x_float * x_float, axis=-1, keepdims=True) + eps_norm)
    hidden_one = x_float + dot(context, full_out)
    scale_two = lax.rsqrt(jnp.mean(hidden_one * hidden_one, axis=-1, keepdims=True) + eps_norm)
    normed_two = (hidden_one * scale_two * gain_two).astype(low)
    normed_float = normed_two.astype(full)
    router_probs = jax.nn.softmax(jnp.dot(normed_float, router, precision=highest), axis=-1)
    picked = jnp.sum(router_probs[:, None, :] * chosen, axis=-1)
    gate_total = jnp.sum(picked, axis=-1, keepdims=True)
    gate_value = picked / gate_total
    combine = gate_value * valid_rows[:, None]
    combine_slots = jnp.sum(
        jnp.where(place_first, combine[None, :, 0], 0.0)
        + jnp.where(place_second, combine[None, :, 1], 0.0),
        axis=1,
    ).reshape(experts, 1, capacity)

    expert_rows = to_experts(dispatch(normed_two)).reshape(-1, width)
    expert_combine = to_experts(combine_slots).reshape(-1, 1)

    gate_part = dot(expert_rows, gate_mine)
    up_part = dot(expert_rows, up_mine)
    active_float, active_pull = jax.vjp(gated_unit, gate_part, up_part)
    active = active_float.astype(low)
    active_scaled = (active_float * expert_combine).astype(low)
    combine_grad_part = jnp.sum(active_float * active_grad_bare, axis=-1).reshape(
        QUAD * experts, 1, capacity
    )
    gate_part_grad, up_part_grad = active_pull(active_grad_bare * expert_combine)
    gate_part_grad = gate_part_grad.astype(low)
    up_part_grad = up_part_grad.astype(low)
    rows_grad_part = (
        lax.dot_general(gate_part_grad, gate_mine, (((1,), (1,)), ((), ())), preferred_element_type=full)
        + lax.dot_general(up_part_grad, up_mine, (((1,), (1,)), ((), ())), preferred_element_type=full)
    ).astype(low)
    output_part = dot(active, down_mine).astype(low)

    combine_grad_back = swap(combine_grad_part, PLANE)
    rows_grad_back = swap(rows_grad_part.reshape(QUAD * experts, capacity, width), PLANE)
    output_back = swap(output_part.reshape(QUAD * experts, capacity, width), PLANE)

    def transposed_dot(a, b):
        return lax.dot_general(a, b, (((0,), (0,)), ((), ())), preferred_element_type=full)

    down_grad = transposed_dot(active_scaled, expert_upstream).astype(low)
    gate_grad = transposed_dot(expert_rows, gate_part_grad).astype(low)
    up_grad = transposed_dot(expert_rows, up_part_grad).astype(low)
    down_share = jnp.sum(
        swap(down_grad.reshape(grps, units, width), "grp").astype(full), axis=0
    )[None]

    def in_columns(grad):
        back = swap(grad.reshape(reps, slab, quarter), REP).astype(full)
        back = jnp.sum(back.reshape(grps, QUAD, slab, grps, units), axis=0)
        return jnp.transpose(back, (1, 2, 0, 3)).reshape(slab, grps * QUAD * units)

    in_share = jnp.concatenate([in_columns(gate_grad), in_columns(up_grad)], axis=1)[None]

    def from_slots(placed, parts):
        hot = jnp.broadcast_to(placed.astype(low)[None], (QUAD,) + placed.shape).reshape(-1, rows)
        return lax.dot_general(
            hot, parts.reshape(-1, width), (((0,), (0,)), ((), ())), preferred_element_type=full
        )

    mixture = combine[:, :1] * from_slots(place_first, output_back) + combine[:, 1:] * from_slots(
        place_second, output_back
    )
    block_loader = (valid_rows[:, None] * (hidden_one + mixture)).astype(low)
    seq_ids = jnp.arange(deal.shape[0], dtype=jnp.int32)
    dealt_seq = jnp.sum(jnp.where(deal == me, seq_ids, 0))
    block_out = lax.dynamic_index_in_dim(
        spread(block_loader, "exp"), dealt_seq - base, 0, keepdims=False
    )

    combine_grad_slots = jnp.sum(combine_grad_back.reshape(QUAD, slots), axis=0)
    combine_grad = jnp.stack(
        [
            jnp.sum(jnp.where(place_first, combine_grad_slots[:, None], 0.0), axis=0),
            jnp.sum(jnp.where(place_second, combine_grad_slots[:, None], 0.0), axis=0),
        ],
        axis=1,
    )
    gate_grad_value = combine_grad * valid_rows[:, None]
    picked_grad = (
        gate_grad_value - jnp.sum(gate_grad_value * gate_value, axis=-1, keepdims=True)
    ) / gate_total
    probs_grad = jnp.sum(picked_grad[:, :, None] * chosen, axis=1)
    logit_grad = router_probs * (
        probs_grad - jnp.sum(probs_grad * router_probs, axis=-1, keepdims=True)
    )
    router_grad = jnp.dot(normed_float.T, logit_grad, precision=highest)
    normed_grad = jnp.dot(logit_grad, router.T, precision=highest) + from_slots(
        jnp.logical_or(place_first, place_second), rows_grad_back
    )
    scaled_two = normed_grad * gain_two
    hidden_grad = (
        upstream
        + scale_two * scaled_two
        - hidden_one * scale_two**3 * jnp.mean(scaled_two * hidden_one, axis=-1, keepdims=True)
    )
    gain_two_grad = jnp.sum(normed_grad * hidden_one * scale_two, axis=0)
    branch_grad = hidden_grad.astype(low)
    context_grad = lax.dot_general(
        branch_grad, full_out, (((1,), (1,)), ((), ())), preferred_element_type=full
    ).astype(low)
    context_grad_pieces = jnp.transpose(context_grad.reshape(rows, exps, head_cols), (1, 0, 2))
    context_grad_mine = swap(context_grad_pieces, "exp").reshape(exps, rows, heads, head_dim)
    branch_group = spread(branch_grad, "exp").reshape(exps * rows, width)
    out_grad = transposed_dot(context_mine.reshape(exps * rows, head_cols), branch_group).astype(low)

    scores = scores_of()
    probs_again = jnp.exp(scores - log_total)
    weights_again = probs_again.astype(low)
    values_grad = jnp.einsum(
        "shij,sihd->sjhd", weights_again, context_grad_mine, preferred_element_type=full
    )
    probs_grad_att = jnp.einsum(
        "sihd,sjhd->shij", context_grad_mine, values, preferred_element_type=full
    )
    row_delta = jnp.sum(probs_grad_att * probs_again, axis=-1, keepdims=True)
    scores_grad = (probs_again * (probs_grad_att - row_delta)).astype(low)
    scores_grad_sum = jnp.sum(scores_grad.astype(full), axis=0)
    bias_grad_mine = jnp.einsum("hij,ijb->bh", scores_grad_sum, onehot, precision=highest)
    bias_grad = lax.dynamic_update_slice_in_dim(
        jnp.zeros((BUCKETS, HEADS), full), bias_grad_mine, place * heads, 1
    )
    queries_grad = (
        jnp.einsum("shij,sjhd->sihd", scores_grad, key_rows, preferred_element_type=full)
        * score_scale
    )
    keys_grad = (
        jnp.einsum("shij,sihd->sjhd", scores_grad, queries, preferred_element_type=full)
        * score_scale
    )
    qkv_grad = (
        jnp.stack([queries_grad, keys_grad, values_grad], axis=2)
        .astype(low)
        .reshape(exps * rows, 3 * head_cols)
    )
    normed_one_part = lax.dot_general(
        qkv_grad, qkv_mine, (((1,), (1,)), ((), ())), preferred_element_type=full
    ).astype(low)
    normed_one_grad = jnp.sum(
        swap(normed_one_part.reshape(exps, rows, width), "exp").astype(full), axis=0
    )
    scaled_one = normed_one_grad * gain_one
    token_grad = (
        hidden_grad
        + scale_one * scaled_one
        - x_float * scale_one**3 * jnp.mean(scaled_one * x_float, axis=-1, keepdims=True)
    )
    gain_one_grad = jnp.sum(normed_one_grad * x_float * scale_one, axis=0)

    qkv_weight_grad = transposed_dot(normed_group, qkv_grad).astype(low)
    qkv_grad_rows = swap(qkv_weight_grad.reshape(exps, row_block, 3 * head_cols), "exp")
    qkv_grad_rows = jnp.transpose(
        qkv_grad_rows.reshape(exps, row_block, 3, head_cols), (1, 2, 0, 3)
    ).reshape(row_block, reps, -1)
    qkv_share = jnp.sum(
        swap(jnp.transpose(qkv_grad_rows, (1, 0, 2)), REP).astype(full), axis=0
    )
    out_pieces = jnp.transpose(out_grad.reshape(row_block, reps, -1), (1, 0, 2))
    out_share = jnp.sum(swap(out_pieces, REP).astype(full), axis=0)

    small = jnp.concatenate(
        [
            router_grad.reshape(-1),
            jnp.stack([gain_one_grad, gain_two_grad], axis=1).reshape(-1),
            bias_grad.reshape(-1),
        ]
    ).reshape(-1, 128)
    small_total = jnp.sum(lax.all_gather(small, ALL, axis=0, tiled=False), axis=0).reshape(-1)
    router_total = small_total[: router.size].reshape(router.shape)
    gains_total = small_total[router.size : router.size + norm_gains.size].reshape(norm_gains.shape)
    bias_total = small_total[router.size + norm_gains.size :].reshape(rel_bias.shape)

    qkv_new = adamw_update(attn_qkv, qkv_first, qkv_second, qkv_share, 1.5 / math.sqrt(D), 0.1)
    out_new = adamw_update(attn_out, out_first, out_second, out_share, 6.0 / math.sqrt(D), 0.1)
    bias_new = adamw_update(rel_bias, bias_first, bias_second, bias_total, 0.3, 0.0)
    router_new = adamw_update(
        router, router_first, router_second, router_total, 1.0 / math.sqrt(D), 0.1
    )
    gains_new = adamw_update(norm_gains, gains_first, gains_second, gains_total, 0.5, 0.0)
    in_new = adamw_update(expert_in, in_first, in_second, in_share, 1.5 / math.sqrt(D), 0.1)
    down_new = adamw_update(
        expert_out, down_first, down_second, down_share, 1.5 / math.sqrt(FF), 0.1
    )
    return (
        (block_out, token_grad)
        + qkv_new
        + out_new
        + bias_new
        + router_new
        + gains_new
        + in_new
        + down_new
    )


def solution(mesh):
    reps, exps = mesh.devices.shape
    split = Mesh(mesh.devices.reshape(reps // QUAD, QUAD, exps), ALL)
    by_rows = P(ALL, None)
    attn = P("exp", REP)
    expert = P("exp", REP, None)
    return jax.shard_map(
        per_device if (reps, exps) == (2 * QUAD, 4) else plain_device,
        mesh=split,
        in_specs=(by_rows, by_rows) + (P(),) * 3 + (attn,) * 6 + (P(),) * 9 + (expert,) * 6,
        out_specs=(by_rows, by_rows) + (attn,) * 6 + (P(),) * 9 + (expert,) * 6,
        check_vma=False,
    )
```

```python
import functools
import math

import jax
import jax.numpy as jnp
from jax import lax
from jax.experimental import pallas as pl
from jax.experimental.pallas import tpu as pltpu
from jax.sharding import Mesh
from jax.sharding import PartitionSpec as P

D = 1024
HEADS = 16
FF = 2816
BUCKETS = 32
STEP = 10
QUAD = 4
REP = ("grp", "quad")
PLANE = ("quad", "exp")
ALL = ("grp", "quad", "exp")

highest = lax.Precision.HIGHEST
eps_norm = 1e-06
thresholds = (1, 2, 3, 4, 5, 6, 7, 8, 11, 16, 22, 32, 45, 64, 90)
beta_one = 0.9
beta_two = 0.999
eps_adam = 1e-08
low = jnp.bfloat16
full = jnp.float32
MESH = pl.DeviceIdType.MESH


def adamw_update(weight, moment, second, gradient, step_rate, decay_factor):
    new_moment = beta_one * moment + (1.0 - beta_one) * gradient
    new_second = beta_two * second + (1.0 - beta_two) * gradient * gradient
    corrected = new_moment / (1.0 - beta_one**STEP)
    scaled = new_second / (1.0 - beta_two**STEP)
    new_weight = weight - step_rate * (
        corrected / (jnp.sqrt(scaled) + eps_adam) + decay_factor * weight
    )
    return (new_moment, new_second, new_weight)


def gated_unit(gate_input, up_input):
    return jax.nn.gelu(gate_input, approximate=True) * up_input


def dot(a, b):
    return jnp.dot(a, b, preferred_element_type=full)


def nt(a, b, precision=None):
    return lax.dot_general(a, b, (((1,), (1,)), ((), ())), preferred_element_type=full, precision=precision)


def tn(a, b):
    return lax.dot_general(a, b, (((0,), (0,)), ((), ())), preferred_element_type=full)


class Where:
    def __init__(self, grps, exps):
        self.grps, self.exps = grps, exps
        self.reps = grps * QUAD
        self.grp = lax.axis_index("grp")
        self.quad = lax.axis_index("quad")
        self.exp = lax.axis_index("exp")
        self.rep = self.grp * QUAD + self.quad
        self.base = self.rep * exps
        self.me = self.base + self.exp

    def device(self, rep, exp):
        return (rep // QUAD, rep % QUAD, exp)

    def near(self, flip):
        q = self.quad
        if flip & 1:
            q = q + 1 - 2 * (q % 2)
        if flip & 2:
            q = q + 2 - 4 * (q // 2)
        return q


def send(src, dst, send_sem, recv_sem, device):
    return pltpu.make_async_remote_copy(
        src_ref=src, dst_ref=dst, send_sem=send_sem, recv_sem=recv_sem, device_id=device, device_id_type=MESH
    )


def arrived(ref, sem):
    pltpu.make_async_copy(ref, ref, sem).wait()


def greet(count, device):
    barrier = pltpu.get_barrier_semaphore()

    def one(k, _):
        pl.semaphore_signal(barrier, inc=1, device_id=device(k), device_id_type=MESH)
        return 0

    lax.fori_loop(1, count + 1, one, 0)
    return functools.partial(pl.semaphore_wait, barrier, count)


def everyone(at):
    count = at.reps * at.exps

    def device(k):
        other = (at.me + k) % count
        return at.device(other // at.exps, other % at.exps)

    return count - 1, device


def neighbours(at):
    members = QUAD * at.exps
    plane = at.quad * at.exps + at.exp

    def device(k):
        other = (plane + k) % members
        rest = k - members
        grp = jnp.where(k < members, at.grp, (at.grp + 1 + rest // QUAD) % at.grps)
        quad = jnp.where(k < members, other // at.exps, rest % QUAD)
        return grp, quad, jnp.where(k < members, other % at.exps, at.exp)

    return members - 1 + QUAD * (at.grps - 1), device


def turn(exp, i):
    beside = exp + 1 - 2 * (exp % 2)
    return jnp.where(i == 0, (beside + 2) % 4, jnp.where(i == 1, (exp + 2) % 4, jnp.where(i == 2, beside, exp)))


def lane_of(shape):
    return lax.broadcasted_iota(jnp.int32, shape, 1)


def row_of(shape):
    return lax.broadcasted_iota(jnp.int32, shape, 0)


def bucket_of(offset):
    distance = jnp.abs(offset)
    bucket = jnp.where(offset > 0, 16, 0)
    for threshold in thresholds:
        bucket = bucket + jnp.where(distance >= threshold, 1, 0)
    return bucket


def bits_of(count):
    return count.bit_length() - 1


def column_parts(width):
    tiles = width // 128
    cuts = [0, (tiles + 2) // 3, (2 * tiles + 2) // 3, tiles]
    return [(cuts[i] * 128, (cuts[i + 1] - cuts[i]) * 128) for i in range(3)]


def flipped(place, bit):
    return place + (1 - 2 * ((place // (1 << bit)) % 2)) * (1 << bit)


class Doubling:
    def __init__(self, at, own, every, sems, core_sems, orders):
        self.at, self.own, self.every = at, own, every
        self.sems, self.core_sems, self.orders = sems, core_sems, orders
        self.plane = at.quad * at.exps + at.exp
        self.steps = len(orders[0])
        self.parts = column_parts(own.shape[1])

    def device(self, bit):
        other = flipped(self.plane, bit)
        return (self.at.grp, other // self.at.exps, other % self.at.exps)

    def place(self, part, j):
        p = self.plane
        for i, bit in enumerate(self.orders[part]):
            if (j >> i) & 1:
                p = flipped(p, bit + 1)
        return p

    def block(self, part, p):
        begin, size = self.parts[part]
        return self.every.at[p, :, pl.ds(begin, size)]

    def source(self, part, j):
        begin, size = self.parts[part]
        return self.own.at[:, pl.ds(begin, size)] if j == 0 else self.block(part, self.place(part, j))

    def index(self, step, part, j):
        return part * (1 << self.steps) + (1 << step) - 1 + j

    def copy(self, step, part, j):
        i = self.index(step, part, j)
        return send(
            self.source(part, j),
            self.block(part, self.place(part, j)),
            self.sems.at[0, i],
            self.sems.at[1, i],
            self.device(self.orders[part][step] + 1),
        )

    def core_copy(self, part, j):
        i = part * (1 << self.steps) + j
        return send(
            self.source(part, j),
            self.block(part, self.place(part, j)),
            self.core_sems.at[0, i],
            self.core_sems.at[1, i],
            self.device(0),
        )

    def start(self):
        for part in range(3):
            for step in range(self.steps):
                self.copy(step, part, 0).start()
        for part in range(3):
            self.core_copy(part, 0).start()
        self.keep().start()

    def keep(self):
        return pltpu.make_async_copy(self.own, self.every.at[self.plane], self.core_sems.at[1, 3 << self.steps])

    def next(self, step):
        for part in range(3):
            for j in range(1 << step):
                k = (1 << step) + j
                arrived(self.block(part, self.place(part, k)), self.sems.at[1, self.index(step, part, j)])
                for later in range(step + 1, self.steps):
                    self.copy(later, part, k).start()
                self.core_copy(part, k).start()

    def finish_in(self):
        for part in range(3):
            for j in range(1 << self.steps):
                there = self.block(part, flipped(self.place(part, j), 0))
                arrived(there, self.core_sems.at[1, part * (1 << self.steps) + j])
        self.keep().wait()

    def finish_out(self):
        for part in range(3):
            for j in range(1 << self.steps):
                self.core_copy(part, j).wait_send()
            for step in range(self.steps):
                for j in range(1 << step):
                    self.copy(step, part, j).wait_send()


class Halving:
    def __init__(self, at, bufs, sems, orders):
        self.at, self.bufs, self.sems = at, bufs, sems
        self.plane = at.quad * at.exps + at.exp
        self.places = bits_of(QUAD * at.exps)
        self.chip_bits = list(range(self.places - 1))
        self.parts = column_parts(bufs[0].shape[2])
        self.orders = orders

    def device(self, bit):
        other = flipped(self.plane, bit)
        return (self.at.grp, other // self.at.exps, other % self.at.exps)

    def hop(self, step, part):
        order = self.orders[part]
        bit = order[step]
        left = [b for b in self.chip_bits if b not in order[:step]]
        pos = left.index(bit)
        half = 1 << (len(left) - 1)
        mine = (self.plane // (1 << (bit + 1))) % 2
        device = self.device(bit + 1)
        begin, size = self.parts[part]
        cols = pl.ds(begin, size)
        base = self.base(step, part)

        def index(j, value):
            return (j >> pos) * (1 << (pos + 1)) + value * (1 << pos) + j % (1 << pos)

        pairs = []
        for j in range(half):
            copy = functools.partial(
                send,
                self.bufs[step].at[index(j, 1 - mine), :, cols],
                self.bufs[step + 1].at[j, :, cols],
                self.sems.at[0, base + j],
                self.sems.at[1, base + j],
                device,
            )
            pairs.append((copy, index(j, mine), j))
        return pairs, begin, size, base

    def base(self, step, part):
        n = len(self.chip_bits)
        return part * (1 << n) + sum(1 << (n - 1 - s) for s in range(step))

    def start(self, step, part=None):
        for p in range(3) if part is None else [part]:
            for copy, _, _ in self.hop(step, p)[0]:
                copy().start()

    def add(self, step, part):
        pairs, begin, size, base = self.hop(step, part)
        cols = pl.ds(begin, size)
        here, there = self.bufs[step], self.bufs[step + 1]
        for _, keep, j in pairs:
            arrived(there.at[j, :, cols], self.sems.at[1, base + j])
            there[j, :, begin : begin + size] = (
                there[j, :, begin : begin + size] + here[keep, :, begin : begin + size]
            )

    def next(self, step):
        for p in range(3):
            self.add(step, p)
            if step + 1 < len(self.chip_bits):
                self.start(step + 1, p)

    def result(self):
        return self.bufs[len(self.chip_bits)]

    def finish(self):
        for step in range(len(self.chip_bits)):
            for p in range(3):
                for copy, _, _ in self.hop(step, p)[0]:
                    copy().wait_send()


class Group:
    def __init__(self, at, own, every, sems):
        self.at, self.own, self.every, self.sems = at, own, every, sems
        self.beside, self.across = at.exp + 1 - 2 * (at.exp % 2), (at.exp + 2) % 4

    def copy(self, src, index, send_index, device):
        return send(
            src, self.every.at[index], self.sems.at[0, send_index], self.sems.at[1, index], self.at.device(self.at.rep, device)
        )

    def first(self):
        return [
            self.copy(self.own, self.at.exp, 0, self.across),
            self.copy(self.own, self.at.exp, 1, self.beside),
        ]

    def second(self):
        return self.copy(self.every.at[self.across], self.across, 2, self.beside)

    def start(self):
        for copy in self.first():
            copy.start()

    def pass_on(self):
        arrived(self.every.at[self.across], self.sems.at[1, self.across])
        self.second().start()

    def arrive(self):
        for index in (self.beside, (self.beside + 2) % 4):
            arrived(self.every.at[index], self.sems.at[1, index])

    def sent(self):
        for copy in self.first() + [self.second()]:
            copy.wait_send()


class Tiles:
    def __init__(self, units, reps):
        self.units = units
        self.reps = reps
        self.hidden = units * reps
        self.half = self.hidden // 256
        self.wide = (self.half + 1) // 2
        self.count = 3
        self.size = 128 * self.wide // self.count
        self.skip = 128 * (2 * self.wide - self.half)

    def start(self, quad):
        return 128 * (self.half * (quad // 2) + (self.half - self.wide) * (quad % 2))

    def rows(self, tile):
        result = []
        for k in range(QUAD):
            found = None
            for parity in range(2):
                first = self.start(parity) + tile * self.size
                live = first + (self.skip if parity and tile == 0 else 0)
                begin = max(live, k * self.units)
                end = min(first + self.size, (k + 1) * self.units)
                if end > begin:
                    found = (begin - k * self.units, end - begin, parity, begin - first)
            result.append(found)
        return result


class Outward:
    def __init__(self, at, tiles, tile, in_low, down_slab, both_w, down_w, nothing, sems, down_sems):
        self.at, self.tiles, self.tile = at, tiles, tile
        self.in_low, self.down_slab, self.both_w, self.down_w = in_low, down_slab, both_w, down_w
        self.nothing, self.sems, self.down_sems = nothing, sems, down_sems
        self.slab = in_low.shape[0]

    def source(self, quad, section):
        begin = section * self.tiles.hidden + self.tiles.start(quad) + self.tile * self.tiles.size
        return self.in_low.at[:, pl.ds(pl.multiple_of(begin, 128), self.tiles.size)]

    def target(self, rep, section):
        rows = pl.ds(pl.multiple_of(rep * self.slab, self.slab), self.slab)
        return self.both_w.at[rows, pl.ds(section * self.tiles.size, self.tiles.size)]

    def over(self, act, first=1, last=None):
        at = self.at

        def one(k, _):
            other = (at.rep + k) % at.reps
            for section in range(2):
                act(
                    functools.partial(
                        send,
                        self.source(other % QUAD, section),
                        self.target(at.rep, section),
                        self.sems.at[0, section * at.reps + other],
                        self.sems.at[1, section * at.reps + at.rep],
                        at.device(other, at.exp),
                    )
                )
            return 0

        lax.fori_loop(first, last or at.reps, one, 0)

    def over_down(self, act, act_local):
        at = self.at
        for k, piece in enumerate(self.tiles.rows(self.tile)):
            if piece is None:
                continue
            begin, count, parity, to = piece
            quad = 2 * (at.rep // QUAD) + parity
            src, dst = self.down_slab.at[pl.ds(begin, count)], self.down_w.at[pl.ds(to, count)]
            recv = self.down_sems.at[1, at.rep]
            for g in range(at.grps):
                stays = jnp.logical_and(at.grp == g, at.quad == quad)
                ours = at.rep % QUAD == k

                @pl.when(jnp.logical_and(ours, jnp.logical_not(stays)))
                def _():
                    act(functools.partial(send, src, dst, self.down_sems.at[0, g], recv, (g, quad, at.exp)))

                @pl.when(jnp.logical_and(ours, stays))
                def _():
                    act_local(functools.partial(pltpu.make_async_copy, src, dst, recv))

    def blank(self):
        return pltpu.make_async_copy(
            self.nothing, self.down_w.at[pl.ds(0, self.tiles.skip)], self.down_sems.at[1, self.at.reps]
        )

    def start(self, first=1, last=None):
        at = self.at
        self.over(lambda copy: copy().start(), first, last)
        if first > 1:
            return
        self.over_down(lambda copy: copy().start(), lambda copy: copy().start())
        for section in range(2):
            pltpu.make_async_copy(
                self.source(at.quad, section), self.target(at.rep, section), self.sems.at[1, section * at.reps + at.rep]
            ).start()
        if self.tile == 0:

            @pl.when(at.quad % 2 == 1)
            def _():
                self.blank().start()

    def arrive(self):
        at = self.at

        def one(rep, _):
            for section in range(2):
                arrived(self.target(rep, section), self.sems.at[1, section * at.reps + rep])
            return 0

        lax.fori_loop(0, at.reps, one, 0)
        for parity in range(2):

            @pl.when(at.quad % 2 == parity)
            def _():
                for k, piece in enumerate(self.tiles.rows(self.tile)):
                    if piece is not None and piece[2] == parity:
                        source = QUAD * (at.quad // 2) + k
                        arrived(self.down_w.at[pl.ds(piece[3], piece[1])], self.down_sems.at[1, source])
                if parity and self.tile == 0:
                    self.blank().wait()

    def sent(self):
        self.over(lambda copy: copy().wait_send())
        self.over_down(lambda copy: copy().wait_send(), lambda copy: None)


class Homeward:
    def __init__(self, at, tiles, tile, both, down, in_parts, down_parts, sems, down_sems, sections=(0, 1)):
        self.at, self.tiles, self.tile, self.sections = at, tiles, tile, sections
        self.both, self.down, self.in_parts, self.down_parts = both, down, in_parts, down_parts
        self.sems, self.down_sems = sems, down_sems
        self.slab = in_parts.shape[1]

    def target(self, grp, quad, parity, section):
        skip = self.tiles.skip if parity and self.tile == 0 else 0
        to = section * self.tiles.hidden + self.tiles.start(quad) + self.tile * self.tiles.size + skip
        to = to if isinstance(to, int) else pl.multiple_of(to, 128)
        return skip, self.in_parts.at[grp, :, pl.ds(to, self.tiles.size - skip)]

    def copy(self, rep, parity, section, local=False):
        at = self.at
        skip, dst = self.target(at.grp, at.quad, parity, section)
        rows = pl.ds(pl.multiple_of(rep * self.slab, self.slab), self.slab)
        src = self.both.at[rows, pl.ds(section * self.tiles.size + skip, self.tiles.size - skip)]
        recv = self.sems.at[1, section * at.reps + at.rep]
        if local:
            return pltpu.make_async_copy(src, dst, recv)
        return send(src, dst, self.sems.at[0, section * at.reps + rep], recv, at.device(rep, at.exp))

    def over(self, act, act_local):
        at = self.at
        for parity in range(2):

            @pl.when(at.quad % 2 == parity)
            def _():
                def one(k, _):
                    for section in self.sections:
                        act(self.copy((at.rep + k) % at.reps, parity, section))
                    return 0

                lax.fori_loop(1, at.reps, one, 0)
                if act_local:
                    for section in self.sections:
                        act_local(self.copy(at.rep, parity, section, local=True))

    def over_down(self, act, act_local):
        at = self.at
        if self.down is None:
            return
        for k, piece in enumerate(self.tiles.rows(self.tile)):
            if piece is None:
                continue
            begin, count, parity, to = piece
            src, dst = self.down.at[pl.ds(to, count)], self.down_parts.at[at.grp, pl.ds(begin, count)]
            recv = self.down_sems.at[1, at.grp]
            stays = jnp.logical_and(at.grp == at.quad // 2, at.quad == k)
            ours = at.quad % 2 == parity

            @pl.when(jnp.logical_and(ours, jnp.logical_not(stays)))
            def _():
                act(functools.partial(send, src, dst, self.down_sems.at[0, k], recv, (at.quad // 2, k, at.exp)))

            @pl.when(jnp.logical_and(ours, stays))
            def _():
                act_local(functools.partial(pltpu.make_async_copy, src, dst, recv))

    def start(self):
        self.over_down(lambda copy: copy().start(), lambda copy: copy().start())
        self.over(lambda copy: copy.start(), lambda copy: copy.start())

    def arrive(self):
        at = self.at
        for rep in range(at.reps):
            for section in self.sections:
                _, dst = self.target(rep // QUAD, rep % QUAD, rep % 2, section)
                arrived(dst, self.sems.at[1, section * at.reps + rep])
        for k, piece in enumerate(self.tiles.rows(self.tile)):
            if piece is None or self.down is None:
                continue

            @pl.when(at.quad == k)
            def _():
                for g in range(at.grps):
                    arrived(self.down_parts.at[g, pl.ds(piece[0], piece[1])], self.down_sems.at[1, g])

    def sent(self):
        self.over(lambda copy: copy.wait_send(), None)
        self.over_down(lambda copy: copy().wait_send(), lambda copy: None)


def forward_kernel(
    grps,
    exps,
    lengths,
    bias_table,
    routes_t,
    tokens,
    cotangent,
    gains,
    router,
    attn_qkv,
    attn_out,
    expert_in,
    expert_out,
    both_w,
    down_w,
    cot_all,
    n_all,
    comb_all,
    qkv_out,
    pb_out,
    mine_out,
    n1_out,
    wqkv_out,
    wout_out,
    h1_out,
    n2_out,
    probs_out,
    in_out,
    down_out,
    in_wide,
    down_wide,
    qkv_t,
    out_w,
    in_low,
    down_slab,
    tok_all,
    wqkv,
    wout,
    n1,
    qkv,
    pb,
    mine,
    ctx,
    bias,
    comb_send,
    nothing,
    tok_sem,
    wq_sem,
    wo_sem,
    wo2_sem,
    weight_sem,
    down_sem,
    ctx_sem,
    cot_sem,
    cot_core_sem,
    n_sem,
    n_core_sem,
    comb_sem,
    store_sem,
    cast_sem,
):
    at = Where(grps, exps)
    reps = at.reps
    rows, width = tokens.shape
    heads = HEADS // exps
    head_dim = width // HEADS
    head_cols = heads * head_dim
    block_cols = min(128, head_cols)
    shard_cols, row_block = qkv_t.shape
    seg = math.gcd(shard_cols, head_cols)
    segs = shard_cols // seg
    tiles = Tiles(down_slab.shape[0], reps)
    plane = at.quad * exps + at.exp
    members = QUAD * exps
    scale = 1.0 / math.sqrt(head_dim)
    SEND, RECV = 0, 1

    met = greet(*everyone(at))
    wide_copies = [
        pltpu.make_async_copy(expert_in, in_wide, cast_sem.at[0]),
        pltpu.make_async_copy(expert_out, down_wide, cast_sem.at[1]),
    ]
    for copy in wide_copies:
        copy.start()
    qkv_t[...] = attn_qkv[...].T.astype(low)
    out_w[...] = attn_out[...].astype(low)
    met()

    def exp_peer(k):
        return (at.exp + k) % exps

    group_tokens = Group(at, tokens, tok_all, tok_sem)
    group_tokens.start()
    tok_all[at.exp] = tokens[...]

    def segment(k):
        col = (at.rep * segs + k) * seg
        section = col // width
        within = col - section * width
        owner = within // head_cols
        return owner, section * head_cols + within - owner * head_cols

    def segment_copy(k, shift):
        owner, offset = segment(k)
        src = qkv_t.at[pl.ds(k * seg, seg)]
        dst = wqkv.at[at.exp, pl.ds(pl.multiple_of(offset, seg), seg)]
        target = at.device((at.rep + shift) % reps, owner)
        return owner, src, dst, functools.partial(
            send, src, dst, wq_sem.at[SEND, k * reps + shift], wq_sem.at[RECV, at.exp * 3 * (head_cols // seg) + offset // seg], target
        )

    def over_segments(act, act_local):
        def one(i, _):
            k, shift = i // reps, i % reps
            owner, src, dst, copy = segment_copy(k, shift)
            stays = jnp.logical_and(shift == 0, owner == at.exp)

            @pl.when(jnp.logical_not(stays))
            def _():
                act(copy())

            @pl.when(stays)
            def _():
                act_local(k, src, dst)

            return 0

        lax.fori_loop(0, segs * reps, one, 0)

    def local_segment(k, src, dst):
        _, offset = segment(k)
        pltpu.make_async_copy(src, dst, wq_sem.at[RECV, at.exp * 3 * (head_cols // seg) + offset // seg]).start()

    over_segments(lambda copy: copy.start(), local_segment)

    for k in range(1, reps):
        other = (at.rep + k) % reps
        send(
            out_w, wout.at[at.exp, at.rep], wo_sem.at[SEND, other], wo_sem.at[RECV, at.rep], at.device(other, at.exp)
        ).start()
    wout[at.exp, at.rep] = out_w[...]
    chip_bits = list(range(bits_of(members) - 1))
    cots = Doubling(at, cotangent, cot_all, cot_sem, cot_core_sem, [chip_bits[::-1]] * 3)
    cots.start()

    span = 2 * rows
    bucket = bucket_of(lane_of((8, span)) - rows)
    for h in range(heads):
        line = jnp.zeros((8, span), full)
        for b in range(BUCKETS):
            line = jnp.where(bucket == b, bias_table[at.exp * heads + h, b], line)
        whole = jnp.broadcast_to(line[0:1], (rows, span))
        bias[h] = pltpu.roll(whole, 0, 1, stride=1, stride_axis=0)[:, rows:]

    group_tokens.pass_on()
    group_tokens.arrive()

    def norm_group(s, _):
        x = tok_all[s].astype(full)
        r = lax.rsqrt(jnp.mean(x * x, axis=1, keepdims=True) + eps_norm)
        n1[s] = (x * r * gains[0:1, :]).astype(low)
        return 0

    lax.fori_loop(0, exps, norm_group, 0)

    for copy in wide_copies:
        copy.wait()
    in_low[...] = in_wide[...].astype(low)
    down_slab[...] = down_wide[...].astype(low)
    nothing[...] = jnp.zeros_like(nothing)
    weights = [
        Outward(
            at, tiles, t, in_low, down_slab, both_w.at[t], down_w.at[t], nothing, weight_sem.at[t], down_sem.at[t]
        )
        for t in range(2)
    ]

    weights[0].start()

    def wait_segment(i, _):
        e, j = i // (3 * head_cols // seg), i % (3 * head_cols // seg)
        arrived(wqkv.at[e, pl.ds(pl.multiple_of(j * seg, seg), seg)], wq_sem.at[RECV, i])
        return 0

    lax.fori_loop(0, exps * 3 * head_cols // seg, wait_segment, 0)

    def project(s, _):
        total = jnp.zeros((rows, 3 * head_cols), full)
        for e in range(exps):
            total = total + nt(n1[s, :, e * row_block : (e + 1) * row_block], wqkv[e])
        qkv[s] = total.astype(low)
        return 0

    lax.fori_loop(0, exps, project, 0)

    group_wout = Group(at, wout.at[at.exp], wout, wo2_sem)

    def beside(k):
        if k == 1:
            for j in range(1, reps):
                other = (at.rep + j) % reps
                arrived(wout.at[at.exp, other], wo_sem.at[RECV, other])
            group_wout.start()
        elif k == 2:
            cots.next(0)
        else:
            group_wout.pass_on()

    def attend(i, _):
        s = turn(at.exp, i)
        for k in range(1, exps):

            @pl.when(i == k)
            def _():
                beside(k)

        ok = lane_of((rows, rows)) < lengths[at.base + s]
        lane = lane_of((rows, block_cols))
        for c in range(head_cols // block_cols):
            cols = slice(c * block_cols, (c + 1) * block_cols)
            q = qkv[s, :, cols] * scale
            k = qkv[s, :, head_cols + c * block_cols : head_cols + (c + 1) * block_cols]
            v = qkv[s, :, 2 * head_cols + c * block_cols : 2 * head_cols + (c + 1) * block_cols]
            result = jnp.zeros((rows, block_cols), full)
            for t in range(block_cols // head_dim):
                h = c * (block_cols // head_dim) + t
                here = jnp.logical_and(lane >= t * head_dim, lane < (t + 1) * head_dim)
                scores = nt(jnp.where(here, q, jnp.zeros_like(q)), k) + bias[h]
                scores = jnp.where(ok, scores, -1e30)
                top = jnp.max(scores, axis=1, keepdims=True)
                weights = jnp.exp(scores - top)
                total = jnp.sum(weights, axis=1, keepdims=True)
                weights = (weights * (1.0 / total)).astype(low)
                result = jnp.where(here, jnp.dot(weights, v, preferred_element_type=full), result)
                pb[s * heads + h] = weights
            mine[s, :, cols] = result.astype(low)

        @pl.when(i < exps - 1)
        def _():
            send(
                mine.at[s], ctx.at[at.exp], ctx_sem.at[SEND, s], ctx_sem.at[RECV, at.exp], at.device(at.rep, s)
            ).start()

        @pl.when(i == exps - 1)
        def _():
            pltpu.make_async_copy(mine.at[s], ctx.at[at.exp], ctx_sem.at[RECV, at.exp]).start()

        return 0

    lax.fori_loop(0, exps, attend, 0)

    cots.next(1)
    group_wout.arrive()
    for e in range(exps):
        arrived(ctx.at[e], ctx_sem.at[RECV, e])

    out_cols = wout.shape[3]
    for r in range(reps):
        cols = slice(r * out_cols, (r + 1) * out_cols)
        total = tokens[:, cols].astype(full)
        for e in range(exps):
            total = total + jnp.dot(ctx[e], wout[e, r], preferred_element_type=full)
        h1_out[:, cols] = total
    h1 = h1_out[...]
    r2 = lax.rsqrt(jnp.mean(h1 * h1, axis=1, keepdims=True) + eps_norm)
    n2 = (h1 * r2 * gains[1:2, :]).astype(low)
    n2_out[...] = n2
    rotated = [chip_bits[c:] + chip_bits[:c] for c in range(3)]
    rows_two = Doubling(at, n2_out, n_all, n_sem, n_core_sem, rotated)
    rows_two.start()
    weights[1].start(1, 3)

    router_rows = jnp.concatenate([router[...], jnp.zeros((128 - exps, width), full)], axis=0)
    logits = nt(n2.astype(full), router_rows, precision=highest)
    lane = lane_of((rows, 128))
    logits = jnp.where(lane < exps, logits, -1e30)
    probs = jnp.exp(logits - jnp.max(logits, axis=1, keepdims=True))
    probs = probs / jnp.sum(probs, axis=1, keepdims=True)
    probs_out[...] = probs
    picked = jnp.where(routed(routes_t, at.me, rows), probs, 0.0)
    comb = picked / jnp.sum(picked, axis=1, keepdims=True)
    comb = jnp.where(row_of((rows, 1)) < lengths[at.me], comb, 0.0)
    comb_send[...] = comb.T[0 : comb_send.shape[0]]

    def comb_copy(k):
        other = (plane + k) % members
        return send(
            comb_send,
            comb_all.at[plane],
            comb_sem.at[SEND, other],
            comb_sem.at[RECV, plane],
            (at.grp, other // exps, other % exps),
        )

    def start_comb(k, _):
        comb_copy(k).start()
        return 0

    lax.fori_loop(1, members, start_comb, 0)
    pltpu.make_async_copy(comb_send, comb_all.at[plane], comb_sem.at[RECV, plane]).start()
    rows_two.next(0)
    weights[1].start(3, 5)

    stores = [
        (qkv, qkv_out),
        (pb, pb_out),
        (mine, mine_out),
        (n1, n1_out),
        (wqkv, wqkv_out),
        (wout, wout_out),
        (in_low, in_out),
        (down_slab, down_out),
    ]
    for i, (src, dst) in enumerate(stores):
        pltpu.make_async_copy(src, dst, store_sem.at[i]).start()

    rows_two.next(1)
    weights[1].start(5)
    for step in range(2, rows_two.steps):
        rows_two.next(step)
    for step in range(2, cots.steps):
        cots.next(step)

    cots.finish_in()
    rows_two.finish_in()

    def comb_in(k, _):
        arrived(comb_all.at[k], comb_sem.at[RECV, k])
        return 0

    lax.fori_loop(0, members, comb_in, 0)
    for tile in weights:
        tile.arrive()

    for k in range(1, exps):
        peer = exp_peer(k)
        arrived(mine.at[peer], ctx_sem.at[SEND, peer])
    over_segments(lambda copy: copy.wait_send(), lambda k, src, dst: None)
    for k in range(1, reps):
        arrived(out_w, wo_sem.at[SEND, (at.rep + k) % reps])
    group_tokens.sent()
    group_wout.sent()
    cots.finish_out()
    rows_two.finish_out()

    def sent_comb(k, _):
        comb_copy(k).wait_send()
        return 0

    lax.fori_loop(1, members, sent_comb, 0)
    for tile in weights:
        tile.sent()
    for i, (src, dst) in enumerate(stores):
        pltpu.make_async_copy(src, dst, store_sem.at[i]).wait()


def forward_call(
    grps, exps, lengths, bias_table, routes_t, tokens, cotangent, gains, router, attn_qkv, attn_out, expert_in, expert_out
):
    reps = grps * QUAD
    rows, width = tokens.shape
    head_cols = width // exps
    row_block, shard_cols = attn_qkv.shape
    seg = math.gcd(shard_cols, head_cols)
    segs = shard_cols // seg
    units = expert_out.shape[0]
    out_cols = attn_out.shape[1]
    heads = HEADS // exps
    members = QUAD * exps
    tiles = Tiles(units, reps)
    shape = jax.ShapeDtypeStruct
    vmem = pl.BlockSpec(memory_space=pltpu.VMEM)
    smem = pl.BlockSpec(memory_space=pltpu.SMEM)
    hbm = pl.BlockSpec(memory_space=pl.ANY)
    results = [
        (shape((2, width, 2 * tiles.size), low), hbm),
        (shape((2, tiles.size, width), low), hbm),
        (shape((members, rows, width), low), hbm),
        (shape((members, rows, width), low), hbm),
        (shape((members, 8, rows), full), hbm),
        (shape((exps, rows, 3 * head_cols), low), hbm),
        (shape((exps * heads, rows, rows), low), hbm),
        (shape((exps, rows, head_cols), low), hbm),
        (shape((exps, rows, width), low), hbm),
        (shape((exps, 3 * head_cols, row_block), low), hbm),
        (shape((exps, reps, row_block, out_cols), low), hbm),
        (shape((rows, width), full), vmem),
        (shape((rows, width), low), vmem),
        (shape((rows, 128), full), vmem),
        (shape(expert_in.shape, low), hbm),
        (shape(expert_out.shape, low), hbm),
    ]
    dma = pltpu.SemaphoreType.DMA
    chips = members // 2
    return pl.pallas_call(
        functools.partial(forward_kernel, grps, exps),
        out_shape=[r[0] for r in results],
        in_specs=[smem] * 2 + [vmem] * 7 + [hbm] * 2,
        out_specs=[r[1] for r in results],
        scratch_shapes=[
            pltpu.VMEM(expert_in.shape, full),
            pltpu.VMEM(expert_out.shape, full),
            pltpu.VMEM((shard_cols, row_block), low),
            pltpu.VMEM((row_block, out_cols), low),
            pltpu.VMEM(expert_in.shape, low),
            pltpu.VMEM(expert_out.shape, low),
            pltpu.VMEM((exps, rows, width), low),
            pltpu.VMEM((exps, 3 * head_cols, row_block), low),
            pltpu.VMEM((exps, reps, row_block, out_cols), low),
            pltpu.VMEM((exps, rows, width), low),
            pltpu.VMEM((exps, rows, 3 * head_cols), low),
            pltpu.VMEM((exps * heads, rows, rows), low),
            pltpu.VMEM((exps, rows, head_cols), low),
            pltpu.VMEM((exps, rows, head_cols), low),
            pltpu.VMEM((heads, rows, rows), full),
            pltpu.VMEM((8, rows), full),
            pltpu.VMEM((tiles.skip, width), low),
            dma((2, exps)),
            dma((2, max(segs * reps, exps * 3 * head_cols // seg))),
            dma((2, reps)),
            dma((2, exps)),
            dma((2, 2, 2 * reps)),
            dma((2, 2, reps + 1)),
            dma((2, exps)),
            dma((2, 3 * chips)),
            dma((2, 3 * chips + 1)),
            dma((2, 3 * chips)),
            dma((2, 3 * chips + 1)),
            dma((2, members)),
            dma((8,)),
            dma((2,)),
        ],
        compiler_params=pltpu.CompilerParams(
            collective_id=0, has_side_effects=True, vmem_limit_bytes=60 * 1024 * 1024
        ),
        name="forward",
    )(lengths, bias_table, routes_t, tokens, cotangent, gains, router, attn_qkv, attn_out, expert_in, expert_out)


def expert_kernel(
    grps,
    exps,
    cap,
    deal,
    routes_t,
    comb,
    n_all,
    cot_all,
    both_w,
    down_w,
    in_low,
    down_slab,
    h1,
    n_total,
    y_half,
    y_far,
    c_in,
    both_g,
    down_g,
    in_parts,
    down_parts,
    place,
    marks,
    n_rows,
    g_rows,
    both_v,
    down_v,
    raw_n,
    raw_g,
    y_acc,
    n_acc,
    both_d,
    active,
    n_bufs,
    c_sum,
    out_y,
    load_sem,
    raw_sem,
    out_sem,
    in_sem,
    in_down_sem,
    home_sem,
    home_down_sem,
    stage_sem,
    far_sem,
    n_sem,
    c_sem,
):
    at = Where(grps, exps)
    rows, width = n_all.shape[1:]
    tiles = Tiles(down_slab.shape[0], at.reps)
    size = tiles.size
    slots = exps * cap
    members = QUAD * exps
    loads = [pltpu.make_async_copy(both_w.at[t], both_v.at[t], load_sem.at[0, t]) for t in range(2)] + [
        pltpu.make_async_copy(down_w.at[t], down_v.at[t], load_sem.at[1, t]) for t in range(2)
    ]
    for copy in loads:
        copy.start()

    def raw_copies(q):
        here = pl.ds(pl.multiple_of(q * exps, exps), exps)
        return [
            pltpu.make_async_copy(n_all.at[here], raw_n.at[pl.ds(q % 2 * exps, exps)], raw_sem.at[0, q % 2]),
            pltpu.make_async_copy(cot_all.at[here], raw_g.at[pl.ds(q % 2 * exps, exps)], raw_sem.at[1, q % 2]),
        ]

    for copy in raw_copies(0):
        copy.start()

    beside = at.exp + 1 - 2 * (at.exp % 2)
    greet(*neighbours(at))()
    last = tiles.count - 1
    incoming = Outward(
        at, tiles, last, in_low, down_slab, both_v.at[last], down_v.at[last], None, in_sem, in_down_sem
    )
    incoming.start()
    home, home_up = [
        Homeward(
            at, tiles, 0, both_v.at[0], down, in_parts, down_parts, home_sem, home_down_sem, (section,)
        )
        for section, down in ((0, down_v.at[0]), (1, None))
    ]

    earlier = jnp.where(row_of((rows, rows)) < lane_of((rows, rows)), 1.0, 0.0).astype(low)
    slot = row_of((cap, rows)).astype(full)

    def dispatch(q, _):
        @pl.when(q + 1 < QUAD)
        def _():
            for copy in raw_copies(q + 1):
                copy.start()

        for copy in raw_copies(q):
            copy.wait()
        lines = []
        for j in range(exps):
            seq = at.grp * members + q * exps + j
            pair = routes_t[:, pl.ds(pl.multiple_of(seq * rows, rows), rows)]
            lines.append(jnp.logical_or(pair[0:1] == at.exp, pair[1:2] == at.exp))
        lines = [jnp.where(line, 1.0, 0.0) for line in lines] + [jnp.zeros((8 - exps, rows), full)]
        hot_low = jnp.concatenate(lines, axis=0).astype(low)
        before = dot(hot_low, earlier)
        for j in range(exps):
            s = q * exps + j
            inside = jnp.logical_and(slot == before[j : j + 1, :], hot_low[j : j + 1, :].astype(full) > 0.5)
            here = jnp.where(inside, 1.0, 0.0)
            place[s] = here.astype(low)
            g = raw_g[q % 2 * exps]
            for b in range(1, exps):
                g = jnp.where(deal[at.grp * members + s] == at.grp * members + q * exps + b, raw_g[q % 2 * exps + b], g)
            where = pl.ds(pl.multiple_of(s * cap, cap), cap)
            n_rows[where] = dot(here.astype(low), raw_n[q % 2 * exps + j]).astype(low)
            g_rows[where] = dot(here.astype(low), g).astype(low)
            marks[where, 0:1] = jnp.sum(here * comb[s, pl.ds(at.exp, 1), :], axis=1, keepdims=True)
            marks[where, 1:2] = jnp.zeros((cap, 1), full)
        return 0

    lax.fori_loop(0, QUAD, dispatch, 0)
    for copy in loads:
        copy.wait()
    curve = math.sqrt(2.0 / math.pi)

    core = at.exp % 2

    plane = at.quad * exps + at.exp
    sibling = at.device(at.rep, beside)
    dn = Halving(at, n_bufs, n_sem, [[0, 1, 2], [1, 2, 0], [2, 0, 1]])

    def n_copy(j):
        return send(raw_n.at[j], n_bufs[0].at[j], far_sem.at[0, 0, j], far_sem.at[0, 1, j], sibling)

    def y_copies(j):
        return (
            pltpu.make_async_copy(out_y.at[j % 2], y_half.at[j], out_sem.at[j % 2]),
            send(raw_n.at[j], y_far.at[j], far_sem.at[1, 0, j], far_sem.at[1, 1, j], sibling),
        )

    def c_copy(k):
        other = (plane + k) % members
        return send(
            c_sum.at[other],
            c_in.at[plane],
            c_sem.at[0, other],
            c_sem.at[1, plane],
            (at.grp, other // exps, other % exps),
        )

    def slots_of(s):
        return pl.ds(pl.multiple_of(s * cap, cap), cap)

    def n_rows_of(s):
        where = slots_of(s)
        line = jnp.sum(place[s].astype(full) * marks[where, 1:2], axis=0, keepdims=True)
        c_sum[s] = jnp.broadcast_to(line, (8, rows))
        return tn(place[s], n_acc[where]).astype(low)

    def y_rows_of(p):
        first = p // exps * exps
        spot = at.grp * members + p
        here, y = place[first], y_acc[slots_of(first)]
        for c in range(1, exps):
            taken = deal[at.grp * members + first + c] == spot
            here = jnp.where(taken, place[first + c], here)
            y = jnp.where(taken, y_acc[slots_of(first + c)], y)
        return (tn(here, y) + jnp.where(deal[at.me] == spot, h1[...], 0.0)).astype(low)

    def give_n(j):
        raw_n[j] = n_rows_of(2 * j + 1 - core)
        n_copy(j).start()
        raw_g[j] = n_rows_of(2 * j + core)

    def add_n(quad):
        for k in range(exps // 2):
            j = quad * (exps // 2) + k
            arrived(n_bufs[0].at[j], far_sem.at[0, 1, j])
            n_bufs[0][j] = n_bufs[0][j] + raw_g[j]

    def give_y(j, _):
        @pl.when(j >= 2)
        def _():
            y_copies(j - 2)[0].wait()

        out_y[j % 2] = y_rows_of(2 * j + core)
        n_copy(j).wait_send()
        raw_n[j] = y_rows_of(2 * j + 1 - core)
        for copy in y_copies(j):
            copy.start()
        return 0

    def start_c(k, _):
        c_copy(k).start()
        return 0

    def tile_work(f, _):
        @pl.when(f == last)
        def _():
            incoming.arrive()
            home.start()

        def chunk(i, _):
            c = jnp.where(i == 0, at.near(3), jnp.where(i == 1, at.near(1), jnp.where(i == 2, at.near(2), at.quad)))
            here = pl.ds(pl.multiple_of(c * slots, slots), slots)
            share = marks[here, 0:1]
            both = dot(n_rows[here], both_v[f])
            gate_part, up_part = both[:, :size], both[:, size:]
            grad = nt(g_rows[here], down_v[f])
            square = gate_part * gate_part
            bend = jnp.tanh(curve * gate_part * (1.0 + 0.044715 * square))
            half = 0.5 * (1.0 + bend)
            gelu = gate_part * half
            slope = half + (0.5 * curve) * gate_part * (1.0 - bend * bend) * (1.0 + (3 * 0.044715) * square)
            value = gelu * up_part
            marks[here, 1:2] += jnp.sum(value * grad, axis=1, keepdims=True)
            grad = grad * share
            active[f % 2, here] = (value * share).astype(low)
            both_d[f % 2, here, :size] = (grad * up_part * slope).astype(low)
            both_d[f % 2, here, size:] = (grad * gelu).astype(low)
            y = dot(active[f % 2, here], down_v[f])
            y_acc[here] = jnp.where(f == 0, y, y_acc[here].astype(full) + y).astype(low)
            n_back = nt(both_d[f % 2, here], both_v[f])
            n_acc[here] = jnp.where(f == 0, n_back, n_acc[here].astype(full) + n_back).astype(low)

            @pl.when(f == last)
            def _():
                for k in range(exps // 2):
                    give_n(c * (exps // 2) + k)

            @pl.when(jnp.logical_and(f == last, i == 2))
            def _():
                add_n(at.near(3))

            @pl.when(jnp.logical_and(f == last, i == 3))
            def _():
                add_n(at.near(1))
                dn.start(0, 1)

            return 0

        lax.fori_loop(0, QUAD, chunk, 0)

        @pl.when(f == 0)
        def _():
            weight_work(0)

        return 0

    def weight_work(f):
        def columns(m, _):
            cols = pl.ds(pl.multiple_of(m * (width // 2), width // 2), width // 2)
            both_v[f, cols] = tn(n_rows[:, cols], both_d[f % 2]).astype(low)
            down_v[f, :, cols] = tn(active[f % 2], g_rows[:, cols]).astype(low)
            return 0

        lax.fori_loop(0, 2, columns, 0)

        for copy in stage_copies(f):
            copy.start()

    def stage_copies(f):
        if f == 0:
            return []
        return [
            pltpu.make_async_copy(both_v.at[f], both_g.at[f - 1], stage_sem.at[0, f]),
            pltpu.make_async_copy(down_v.at[f], down_g.at[f - 1], stage_sem.at[1, f]),
        ]

    lax.fori_loop(0, tiles.count, tile_work, 0)

    half = members // 2
    lax.fori_loop(1, members, start_c, 0)
    c_in[plane] = c_sum[plane]
    weight_work(1)
    add_n(at.near(2))
    dn.start(0, 2)
    add_n(at.quad)
    dn.start(0, 0)
    weight_work(2)
    lax.fori_loop(0, half, give_y, 0)
    dn.next(0)
    home_up.start()
    for step in range(1, len(dn.chip_bits)):
        dn.next(step)
    n_total[...] = dn.result()[0]
    for j in (half - 2, half - 1):
        y_copies(j)[0].wait()
    for f in range(tiles.count):
        for copy in stage_copies(f):
            copy.wait()

    def core_in(j, _):
        y_copies(j)[1].wait_send()
        arrived(y_far.at[j], far_sem.at[1, 1, j])
        return 0

    lax.fori_loop(0, half, core_in, 0)

    def c_done(k, _):
        c_copy(k).wait_send()
        other = (plane + k) % members
        arrived(c_in.at[other], c_sem.at[1, other])
        return 0

    lax.fori_loop(1, members, c_done, 0)
    dn.finish()
    home.arrive()
    home_up.arrive()
    incoming.sent()
    home.sent()
    home_up.sent()


def expert_call(grps, exps, cap, deal, routes_t, comb_all, n_all, cot_all, both_w, down_w, in_low, down_slab, h1):
    members, rows, width = n_all.shape
    reps = grps * QUAD
    tiles = Tiles(down_slab.shape[0], reps)
    size = tiles.size
    slab, both_hidden = in_low.shape
    units = down_slab.shape[0]
    slots = exps * cap
    chip_bits = bits_of(members) - 1
    shape = jax.ShapeDtypeStruct
    vmem = pl.BlockSpec(memory_space=pltpu.VMEM)
    smem = pl.BlockSpec(memory_space=pltpu.SMEM)
    hbm = pl.BlockSpec(memory_space=pl.ANY)
    results = [
        (shape((rows, width), low), vmem),
        (shape((members // 2, rows, width), low), hbm),
        (shape((members // 2, rows, width), low), hbm),
        (shape((members, 8, rows), full), vmem),
        (shape((2, width, 2 * size), low), hbm),
        (shape((2, size, width), low), hbm),
        (shape((grps, slab, both_hidden), low), hbm),
        (shape((grps, units, width), low), hbm),
    ]
    dma = pltpu.SemaphoreType.DMA
    return pl.pallas_call(
        functools.partial(expert_kernel, grps, exps, cap),
        out_shape=[r[0] for r in results],
        in_specs=[smem] + [vmem] * 2 + [hbm] * 6 + [vmem],
        out_specs=[r[1] for r in results],
        scratch_shapes=[
            pltpu.VMEM((members, cap, rows), low),
            pltpu.VMEM((QUAD * slots, 128), full),
            pltpu.VMEM((QUAD * slots, width), low),
            pltpu.VMEM((QUAD * slots, width), low),
            pltpu.VMEM((tiles.count, width, 2 * size), low),
            pltpu.VMEM((tiles.count, size, width), low),
            pltpu.VMEM((2 * exps, rows, width), low),
            pltpu.VMEM((2 * exps, rows, width), low),
            pltpu.VMEM((QUAD * slots, width), low),
            pltpu.VMEM((QUAD * slots, width), low),
            pltpu.VMEM((2, QUAD * slots, 2 * size), low),
            pltpu.VMEM((2, QUAD * slots, size), low),
            [pltpu.VMEM((members >> (1 + step), rows, width), low) for step in range(chip_bits + 1)],
            pltpu.VMEM((members, 8, rows), full),
            pltpu.VMEM((2, rows, width), low),
            dma((2, 2)),
            dma((2, 2)),
            dma((2,)),
            dma((2, 2 * reps)),
            dma((2, reps + 1)),
            dma((2, 2 * reps)),
            dma((2, max(QUAD, grps))),
            dma((2, tiles.count)),
            dma((2, 2, members // 2)),
            dma((2, 3 << chip_bits)),
            dma((2, members)),
        ],
        compiler_params=pltpu.CompilerParams(
            collective_id=2, has_side_effects=True, vmem_limit_bytes=60 * 1024 * 1024
        ),
        name="experts",
    )(deal, routes_t, comb_all, n_all, cot_all, both_w, down_w, in_low, down_slab, h1)


def adamw_root(weight, moment, second, gradient, step_rate, decay_factor):
    new_moment = beta_one * moment + (1.0 - beta_one) * gradient
    new_second = beta_two * second + (1.0 - beta_two) * gradient * gradient
    root = lax.rsqrt(new_second * (1.0 / (1.0 - beta_two**STEP)))
    step = new_moment * (root * (1.0 - eps_adam * root))
    keep = 1.0 - step_rate * decay_factor
    return (new_moment, new_second, keep * weight - (step_rate / (1.0 - beta_one**STEP)) * step)


def adam_kernel(exps, *refs):
    in_parts, down_parts, qkv_grad, out_grad, small = refs[:5]
    states, news, bias_grad = refs[5:26], refs[26:47], refs[47]
    heads = HEADS // exps
    width = small.shape[1]

    def update(i, grad, rate, decay):
        weight, first, second = [state[...] for state in states[3 * i : 3 * i + 3]]
        values = adamw_root(weight, first, second, grad, rate, decay)
        for new, value in zip(news[3 * i : 3 * i + 3], values, strict=True):
            new[...] = value

    def total(parts):
        result = parts[0].astype(full)
        for k in range(1, parts.shape[0]):
            result = result + parts[k].astype(full)
        return result

    @pl.when(pl.program_id(0) == 0)
    def _():
        update(0, qkv_grad[...], 1.5 / math.sqrt(D), 0.1)
        update(1, out_grad[...], 6.0 / math.sqrt(D), 0.1)
        for e in range(exps):
            for h in range(heads):
                bias_grad[e * heads + h : e * heads + h + 1, :] = small[
                    exps + 3 + e : exps + 4 + e, h * 128 : h * 128 + BUCKETS
                ]
        update(2, bias_grad[...], 0.3, 0.0)
        update(3, small[0:exps, :], 1.0 / math.sqrt(D), 0.1)
        update(4, small[exps : exps + 2, :], 0.5, 0.0)

    update(5, total(in_parts), 1.5 / math.sqrt(D), 0.1)
    update(6, total(down_parts), 1.5 / math.sqrt(FF), 0.1)


def adam_call(exps, in_parts, down_parts, qkv_grad, out_grad, small, states):
    steps = 4

    def whole(array):
        return pl.BlockSpec(array.shape, lambda i: (0,) * array.ndim)

    def columns(array):
        block = array.shape[:-1] + (array.shape[-1] // steps,)
        return pl.BlockSpec(block, lambda i: (0,) * (array.ndim - 1) + (i,))

    specs = [whole(state) for state in states[:15]]
    specs += [columns(state) for state in states[15:18]] + [columns(state) for state in states[18:]]
    return pl.pallas_call(
        functools.partial(adam_kernel, exps),
        grid=(steps,),
        in_specs=[columns(in_parts), columns(down_parts), whole(qkv_grad), whole(out_grad), whole(small)] + specs,
        out_specs=specs,
        out_shape=[jax.ShapeDtypeStruct(state.shape, full) for state in states],
        scratch_shapes=[pltpu.VMEM((HEADS, BUCKETS), full)],
        compiler_params=pltpu.CompilerParams(vmem_limit_bytes=60 * 1024 * 1024),
        name="adam",
    )(in_parts, down_parts, qkv_grad, out_grad, small, *states)


def backward_kernel(
    grps,
    exps,
    lengths,
    deal,
    y_half,
    y_far,
    both_g,
    down_g,
    in_before,
    down_before,
    n1_in,
    cot_all,
    routes_t,
    tokens,
    n_total,
    c_in,
    n2_in,
    probs_in,
    h1_from,
    qkv_from,
    pb_from,
    mine_from,
    wqkv_from,
    wout_from,
    gains,
    router_t,
    *rest,
):
    token_grad, block_out, in_parts, down_parts, qkv_grad, out_grad, small_out = rest[:7]
    scratch = rest[7:]
    (
    h1_in,
    qkv,
    pb,
    mine,
    wqkv,
    wout,
    kept,
    y_bufs,
    dh1,
    dz_send,
    dz_all,
    do_send,
    do_in,
    bias_sum,
    dqkv,
    dqkv_t,
    dn1_send,
    dn1_in,
    wq_send,
    og_send,
    mids,
    far_send,
    far_in,
    small_send,
    small_exp,
    small_sum,
    small_rep,
    small_half,
    small_far,
    y_sem,
    load_sem,
    weight_sem,
    down_sem,
    dz_sem,
    do_sem,
    dn1_sem,
    wq_sem,
    og_sem,
    mid_sem,
    far_sem,
    small_sem,
    small2_sem,
    small3_sem,
    n1_sem,
    operand_sem,
    ) = scratch
    at = Where(grps, exps)
    reps = at.reps
    rows, width = tokens.shape
    heads = HEADS // exps
    head_dim = width // HEADS
    head_cols = heads * head_dim
    block_cols = min(128, head_cols)
    row_block = wqkv.shape[2]
    out_cols = wout.shape[3]
    tiles = Tiles(down_parts.shape[1], reps)
    scale = 1.0 / math.sqrt(head_dim)
    SEND, RECV = 0, 1
    plane = at.quad * exps + at.exp
    members = QUAD * exps

    def exp_peer(k):
        return (at.exp + k) % exps

    router = router_t[...]
    met = greet(*neighbours(at))
    n1 = kept.at[0:exps]
    group = pl.ds(pl.multiple_of(at.quad * exps, exps), exps)
    cot_copy = pltpu.make_async_copy(cot_all.at[group], dn1_send, n1_sem.at[1])
    cot_copy.start()
    loads = [
        pltpu.make_async_copy(src, dst, operand_sem.at[i])
        for i, (src, dst) in enumerate(
            ((h1_from, h1_in), (wout_from, wout), (qkv_from, qkv), (pb_from, pb), (mine_from, mine), (wqkv_from, wqkv))
        )
    ]
    ys = Halving(at, y_bufs, y_sem, [[0, 1, 2], [1, 0, 2], [1, 0, 2]])
    half_loads = [
        pltpu.make_async_copy(y_far, y_bufs[0], load_sem.at[0]),
        pltpu.make_async_copy(y_half, kept, load_sem.at[1]),
    ]
    for copy in loads + half_loads:
        copy.start()

    span = 2 * rows
    met()

    homes = [
        Homeward(
            at, tiles, t + 1, both_g.at[t], down, in_parts, down_parts, weight_sem.at[t], down_sem.at[t], sections
        )
        for t, down, sections in ((0, down_g.at[0], (0, 1)), (1, down_g.at[1], (0,)), (1, None, (1,)))
    ]
    homes[0].start()
    n1_copy = pltpu.make_async_copy(n1_in, n1, n1_sem.at[0])

    lane = lane_of((rows, 128))
    comb_rows = []
    for e in range(exps):
        total = c_in[e]
        for q in range(1, QUAD):
            total = total + c_in[q * exps + e]
        comb_rows.append(total[0:1, :])
    comb_rows.append(jnp.zeros((128 - exps, rows), full))
    comb_grad = jnp.concatenate(comb_rows, axis=0).T
    valid = row_of((rows, 1)) < lengths[at.me]
    probs = probs_in[...]
    hot = routed(routes_t, at.me, rows)
    picked = jnp.where(hot, probs, 0.0)
    total = jnp.sum(picked, axis=1, keepdims=True)
    gate = picked / total
    gate_grad_rows = jnp.where(valid, comb_grad, 0.0)
    spread_grad = jnp.sum(gate_grad_rows * gate, axis=1, keepdims=True)
    probs_grad = jnp.where(hot, (gate_grad_rows - spread_grad) / total, 0.0)
    logit_grad = probs * (probs_grad - jnp.sum(probs_grad * probs, axis=1, keepdims=True))
    small_rows = small_send.shape[0]
    small_send[...] = jnp.zeros_like(small_send)
    router_back = jnp.dot(
        logit_grad, jnp.concatenate([router, jnp.zeros((128 - exps, width), full)], axis=0),
        precision=highest, preferred_element_type=full,
    )
    for copy in loads:
        copy.wait()
    h1 = h1_in[...]
    r2 = lax.rsqrt(jnp.mean(h1 * h1, axis=1, keepdims=True) + eps_norm)

    steps = len(ys.chip_bits)
    n2_grad = router_back + n_total[...].astype(full)
    scaled = n2_grad * gains[1:2, :]
    cot_copy.wait()
    dealt = deal[at.me] - at.base
    g = dn1_send[0]
    for e in range(1, exps):
        g = jnp.where(dealt == e, dn1_send[e], g)
    hidden_grad = (
        jnp.where(valid, g.astype(full), 0.0)
        + r2 * scaled
        - h1 * (r2 * r2 * r2) * jnp.mean(scaled * h1, axis=1, keepdims=True)
    )
    dh1[...] = hidden_grad
    small_send[exps + 1 : exps + 2, :] = jnp.sum(n2_grad * h1 * r2, axis=0, keepdims=True)
    branch = hidden_grad.astype(low)
    dz_send[...] = branch
    for e in range(exps):
        total = jnp.zeros((rows, row_block), full)
        for r in range(reps):
            total = total + nt(branch[:, r * out_cols : (r + 1) * out_cols], wout[e, r])
        do_send[e] = total.astype(low)

    def do_copies():
        return [
            send(
                do_send.at[exp_peer(k)],
                do_in.at[at.exp],
                do_sem.at[SEND, exp_peer(k)],
                do_sem.at[RECV, at.exp],
                at.device(at.rep, exp_peer(k)),
            )
            for k in range(1, exps)
        ]

    for copy in do_copies():
        copy.start()
    pltpu.make_async_copy(do_send.at[at.exp], do_in.at[at.exp], do_sem.at[RECV, at.exp]).start()

    group_dz = Group(at, dz_send, dz_all, dz_sem)
    dz_all[at.exp] = branch
    for copy in half_loads:
        copy.wait()

    def add_halves(j, _):
        y_bufs[0][j] = y_bufs[0][j] + kept[j]
        return 0

    lax.fori_loop(0, kept.shape[0], add_halves, 0)
    n1_copy.start()

    bias_sum[...] = jnp.zeros_like(bias_sum)

    def dn1_copies():
        beside, across = turn(at.exp, 2), turn(at.exp, 1)
        return [
            functools.partial(
                send, dn1_send.at[k], dn1_in.at[j], dn1_sem.at[SEND, j], dn1_sem.at[RECV, j], at.device(at.rep, to)
            )
            for k, j, to in ((turn(at.exp, 0), 2, beside), (across, 0, across), (beside, 1, beside))
        ]

    def attend_back(i, _):
        s = turn(at.exp, i)
        arrived(do_in.at[s], do_sem.at[RECV, s])

        @pl.when(i == 0)
        def _():
            group_dz.start()
            ys.start(0)

        @pl.when(i == 1)
        def _():
            homes[1].start()

        @pl.when(i == 2)
        def _():
            group_dz.pass_on()

        block_lane = lane_of((rows, block_cols))
        for c in range(head_cols // block_cols):
            cols = slice(c * block_cols, (c + 1) * block_cols)
            k_cols = slice(head_cols + c * block_cols, head_cols + (c + 1) * block_cols)
            v_cols = slice(2 * head_cols + c * block_cols, 2 * head_cols + (c + 1) * block_cols)
            q = qkv[s, :, cols] * scale
            k = qkv[s, :, k_cols]
            v = qkv[s, :, v_cols]
            do = do_in[s, :, cols]
            dq = jnp.zeros((rows, block_cols), full)
            dk = jnp.zeros((rows, block_cols), full)
            dv = jnp.zeros((rows, block_cols), full)
            for t in range(block_cols // head_dim):
                h = c * (block_cols // head_dim) + t
                here = jnp.logical_and(block_lane >= t * head_dim, block_lane < (t + 1) * head_dim)
                zero = jnp.zeros_like(q)
                do_h = jnp.where(here, do, zero)
                weights = pb[s * heads + h]
                p = weights.astype(full)
                dp = nt(do_h, v)
                delta = jnp.sum(dp * p, axis=1, keepdims=True)
                ds = (p * (dp - delta)).astype(low)
                bias_sum[h] += ds.astype(full)
                dv = jnp.where(here, tn(weights, do), dv)
                dq = jnp.where(here, jnp.dot(ds, k, preferred_element_type=full), dq)
                dk = jnp.where(here, tn(ds, q), dk)
            dqkv[:, cols] = (dq * scale).astype(low)
            dqkv[:, k_cols] = dk.astype(low)
            dqkv[:, v_cols] = dv.astype(low)
        dqkv_t[:, pl.ds(pl.multiple_of(s * rows, rows), rows)] = dqkv[...].T
        for e in range(exps):
            dn1_send[s, :, e * row_block : (e + 1) * row_block] = jnp.dot(
                dqkv[...], wqkv[e], preferred_element_type=full
            ).astype(low)

        @pl.when(i == 0)
        def _():
            dn1_copies()[0]().start()

        @pl.when(i == 1)
        def _():
            arrived(dn1_in.at[2], dn1_sem.at[RECV, 2])
            dn1_send[s] = (dn1_send[s].astype(full) + dn1_in[2].astype(full)).astype(low)
            dn1_copies()[1]().start()

        @pl.when(i == 2)
        def _():
            dn1_copies()[2]().start()

        return 0

    lax.fori_loop(0, exps, attend_back, 0)

    n1_copy.wait()
    seg = wq_send.shape[2]
    parts = wq_send.shape[1]
    segs = mids.shape[1] - 1
    for e in range(exps):
        part = kept[0:exps, :, e * row_block : (e + 1) * row_block].reshape(exps * rows, row_block)
        total = dot(dqkv_t[...], part)
        for j in range(parts):
            wq_send[e, j] = total[j * seg : (j + 1) * seg].astype(low)

    def owner(j):
        section, within = j // (head_cols // seg), j % (head_cols // seg)
        col = section * width + at.exp * head_cols + within * seg
        block = col // seg
        return block // segs, block % segs

    def mid_place(grp, k, quad):
        return (grp * (segs + 1) + k) * QUAD + quad

    def mid_copy(src, send_sem, rep, k, e):
        dst = mids.at[rep // QUAD, k, at.quad]
        recv = mid_sem.at[mid_place(rep // QUAD, k, at.quad)]
        stays = jnp.logical_and(rep % QUAD == at.quad, e == at.exp)
        return (
            stays,
            functools.partial(send, src, dst, send_sem, recv, (at.grp, rep % QUAD, e)),
            functools.partial(pltpu.make_async_copy, src, dst, recv),
        )

    def wq_copy(i):
        e, j = i // parts, i % parts
        rep, k = owner(j)
        return mid_copy(wq_send.at[e, j], wq_sem.at[i], rep, k, e)

    def og_copy(r):
        return mid_copy(og_send.at[r], og_sem.at[r], r, segs, at.exp)

    def go(copies, act, act_local):
        stays, away, local = copies

        @pl.when(jnp.logical_not(stays))
        def _():
            act(away)

        if act_local:

            @pl.when(stays)
            def _():
                act_local(local)

    def over(count, copies, act, act_local):
        def one(i, _):
            go(copies(i), act, act_local)
            return 0

        lax.fori_loop(0, count, one, 0)

    over(exps * parts, wq_copy, lambda copy: copy().start(), lambda copy: copy().start())
    ys.next(0)
    group_dz.arrive()
    grad = tn(mine[...].reshape(exps * rows, head_cols), dz_all[...].reshape(exps * rows, width))
    for r in range(reps):
        og_send[r] = grad[:, r * out_cols : (r + 1) * out_cols].T.astype(low)
    over(reps, og_copy, lambda copy: copy().start(), lambda copy: copy().start())
    homes[2].start()

    n1_grad = dn1_send[at.exp].astype(full)
    for j in range(2):
        arrived(dn1_in.at[j], dn1_sem.at[RECV, j])
        n1_grad = n1_grad + dn1_in[j].astype(full)
    x = tokens[...].astype(full)
    r1 = lax.rsqrt(jnp.mean(x * x, axis=1, keepdims=True) + eps_norm)
    scaled = n1_grad * gains[0:1, :]
    token_grad[...] = (
        dh1[...] + r1 * scaled - x * (r1 * r1 * r1) * jnp.mean(scaled * x, axis=1, keepdims=True)
    )
    small_send[exps : exps + 1, :] = jnp.sum(n1_grad * x * r1, axis=0, keepdims=True)

    ys.next(1)
    router_rows = lax.dot_general(
        logit_grad, n2_in[...].astype(full), (((0,), (0,)), ((), ())), preferred_element_type=full, precision=highest
    )
    small_send[0:exps, :] = router_rows[0:exps, :]

    flip = jnp.where(row_of((rows, rows)) + lane_of((rows, rows)) == rows - 1, 1.0, 0.0).astype(low)
    diagonals = []
    for h in range(heads):
        high = bias_sum[h].astype(low)
        rest = (bias_sum[h] - high.astype(full)).astype(low)
        flipped = dot(high, flip) + dot(rest, flip)
        square = jnp.concatenate([flipped, jnp.zeros((rows, rows), full)], axis=1)
        turned = pltpu.roll(square, 0, 1, stride=1, stride_axis=0)
        diagonals.append(jnp.sum(turned, axis=0, keepdims=True))
    diagonals = jnp.concatenate(diagonals + [jnp.zeros((8 - heads, span), full)], axis=0)
    in_bucket = jnp.where(bucket_of(rows - 1 - row_of((span, 128))) == lane_of((span, 128)), 1.0, 0.0)
    bias_line = jnp.dot(diagonals, in_bucket, precision=highest, preferred_element_type=full)
    for h in range(heads):
        small_send[exps + 2 : exps + 3, h * 128 : (h + 1) * 128] = bias_line[h : h + 1, :]

    def small_copies():
        return [
            send(
                small_send,
                small_exp.at[at.exp],
                small_sem.at[SEND, exp_peer(k)],
                small_sem.at[RECV, at.exp],
                at.device(at.rep, exp_peer(k)),
            )
            for k in range(1, exps)
        ]

    for copy in small_copies():
        copy.start()
    small_exp[at.exp] = small_send[...]

    def mid_sum(grp, k):
        for q in range(QUAD):
            arrived(mids.at[grp, k, q], mid_sem.at[mid_place(grp, k, q)])
        total = mids[grp, k, 0].astype(full)
        for q in range(1, QUAD):
            total = total + mids[grp, k, q].astype(full)
        return total

    far = 1 - at.grp
    for k in range(segs + 1):
        far_send[k] = mid_sum(far, k).astype(low)

    def far_copy():
        return send(far_send, far_in, far_sem.at[SEND], far_sem.at[RECV], (far, at.quad, at.exp))

    far_copy().start()
    for k in range(1, exps):
        arrived(small_exp.at[exp_peer(k)], small_sem.at[RECV, exp_peer(k)])
    total = small_exp[0]
    for e in range(1, exps):
        total = total + small_exp[e]
    small_sum[...] = total
    for e in range(exps):
        small_sum[exps + 3 + e : exps + 4 + e, :] = small_exp[e, exps + 2 : exps + 3, :]

    def small2_copies():
        return [
            send(
                small_sum,
                small_rep.at[at.quad],
                small2_sem.at[SEND, k - 1],
                small2_sem.at[RECV, at.quad],
                (at.grp, (at.quad + k) % QUAD, at.exp),
            )
            for k in range(1, QUAD)
        ]

    def small3_copy():
        return send(small_half, small_far, small3_sem.at[SEND], small3_sem.at[RECV], (far, at.quad, at.exp))

    for copy in small2_copies():
        copy.start()
    small_rep[at.quad] = small_sum[...]
    for step in range(2, steps):
        ys.next(step)
    length = lengths[at.base]
    for e in range(1, exps):
        length = jnp.where(deal[at.base + e] == at.me, lengths[at.base + e], length)
    block = ys.result()[0]
    block_out[...] = jnp.where(row_of((rows, 1)) < length, block, jnp.zeros_like(block))
    for k in range(1, QUAD):
        arrived(small_rep.at[(at.quad + k) % QUAD], small2_sem.at[RECV, (at.quad + k) % QUAD])
    total = small_rep[0]
    for q in range(1, QUAD):
        total = total + small_rep[q]
    small_half[...] = total
    small3_copy().start()
    arrived(small_far, small3_sem.at[RECV])
    total = small_half[...] + small_far[...]
    small_out[...] = total

    near = [mid_sum(at.grp, k) for k in range(segs + 1)]
    arrived(far_in, far_sem.at[RECV])
    grads = [(near[k] + far_in[k].astype(full)).T for k in range(segs + 1)]
    qkv_grad[...] = jnp.concatenate(grads[:segs], axis=1)
    out_grad[...] = grads[segs]
    for home in homes:
        home.arrive()

    ys.finish()

    for home in homes:
        home.sent()

    over(exps * parts, wq_copy, lambda copy: copy().wait_send(), None)
    over(reps, og_copy, lambda copy: copy().wait_send(), None)
    far_copy().wait_send()
    small3_copy().wait_send()
    for copies in (do_copies(), small_copies(), small2_copies()):
        for copy in copies:
            copy.wait_send()
    for copy in dn1_copies():
        copy().wait_send()
    group_dz.sent()


def routed(routes_t, seq, rows):
    pair = routes_t[:, pl.ds(pl.multiple_of(seq * rows, rows), rows)].astype(full)
    cols = jnp.concatenate([pair, jnp.zeros((126, rows), full)], axis=0).T
    lane = lane_of((rows, 128)).astype(full)
    return jnp.logical_or(lane == cols[:, 0:1], lane == cols[:, 1:2])


def backward_call(
    grps, exps, lengths, deal, y_half, y_far, both_g, down_g, in_before, down_before, n1,
    cot_all, routes_t, tokens, n_total, c_in, n2, probs, h1, qkv, pb, mine, wqkv, wout, gains, router
):
    reps = grps * QUAD
    rows, width = tokens.shape
    heads = HEADS // exps
    head_cols = width // exps
    row_block = wqkv.shape[2]
    out_cols = wout.shape[3]
    shard_cols = 3 * width // reps
    seg = math.gcd(shard_cols, head_cols)
    segs = shard_cols // seg
    parts = 3 * head_cols // seg
    members = QUAD * exps
    chip_bits = bits_of(members) - 1
    small_rows = -(-(2 * exps + 3) // 8) * 8
    shape = jax.ShapeDtypeStruct
    vmem = pl.BlockSpec(memory_space=pltpu.VMEM)
    smem = pl.BlockSpec(memory_space=pltpu.SMEM)
    hbm = pl.BlockSpec(memory_space=pl.ANY)
    results = [
        (shape((rows, width), full), vmem),
        (shape((rows, width), low), vmem),
        (shape(in_before.shape, low), hbm),
        (shape(down_before.shape, low), hbm),
        (shape((row_block, shard_cols), full), vmem),
        (shape((row_block, out_cols), full), vmem),
        (shape((small_rows, width), full), vmem),
    ]
    dma = pltpu.SemaphoreType.DMA
    bufs = [pltpu.VMEM((1 << (chip_bits - s), rows, width), low) for s in range(chip_bits + 1)]
    return pl.pallas_call(
        functools.partial(backward_kernel, grps, exps),
        out_shape=[r[0] for r in results],
        in_specs=[smem] * 2 + [hbm] * 8 + [vmem] * 6 + [hbm] * 6 + [vmem] * 2,
        out_specs=[r[1] for r in results],
        scratch_shapes=[
            pltpu.VMEM(h1.shape, full),
            pltpu.VMEM(qkv.shape, low),
            pltpu.VMEM(pb.shape, low),
            pltpu.VMEM(mine.shape, low),
            pltpu.VMEM(wqkv.shape, low),
            pltpu.VMEM(wout.shape, low),
            pltpu.VMEM((members // 2, rows, width), low),
            list(bufs),
            pltpu.VMEM((rows, width), full),
            pltpu.VMEM((rows, width), low),
            pltpu.VMEM((exps, rows, width), low),
            pltpu.VMEM((exps, rows, head_cols), low),
            pltpu.VMEM((exps, rows, head_cols), low),
            pltpu.VMEM((heads, rows, rows), full),
            pltpu.VMEM((rows, 3 * head_cols), low),
            pltpu.VMEM((3 * head_cols, exps * rows), low),
            pltpu.VMEM((exps, rows, width), low),
            pltpu.VMEM((3, rows, width), low),
            pltpu.VMEM((exps, parts, seg, row_block), low),
            pltpu.VMEM((reps, seg, row_block), low),
            pltpu.VMEM((grps, segs + 1, QUAD, seg, row_block), low),
            pltpu.VMEM((segs + 1, seg, row_block), low),
            pltpu.VMEM((segs + 1, seg, row_block), low),
            pltpu.VMEM((small_rows, width), full),
            pltpu.VMEM((exps, small_rows, width), full),
            pltpu.VMEM((small_rows, width), full),
            pltpu.VMEM((QUAD, small_rows, width), full),
            pltpu.VMEM((small_rows, width), full),
            pltpu.VMEM((small_rows, width), full),
            dma((2, 3 << chip_bits)),
            dma((2,)),
            dma((2, 2, 2 * reps)),
            dma((2, 2, max(QUAD, grps))),
            dma((2, exps)),
            dma((2, exps)),
            dma((2, exps)),
            dma((exps * parts,)),
            dma((reps,)),
            dma((grps * (segs + 1) * QUAD,)),
            dma((2,)),
            dma((2, exps)),
            dma((2, QUAD)),
            dma((2,)),
            dma((2,)),
            dma((6,)),
        ],
        compiler_params=pltpu.CompilerParams(
            collective_id=1, has_side_effects=True, vmem_limit_bytes=60 * 1024 * 1024
        ),
        input_output_aliases={6: 2, 7: 3},
        name="backward",
    )(
        lengths, deal, y_half, y_far, both_g, down_g, in_before, down_before, n1, cot_all,
        routes_t, tokens, n_total, c_in, n2, probs, h1, qkv, pb, mine, wqkv, wout, gains, router
    )


def per_device(
    tokens,
    cotangent,
    seq_lengths,
    deal,
    routes,
    attn_qkv,
    qkv_first,
    qkv_second,
    attn_out,
    out_first,
    out_second,
    rel_bias,
    bias_first,
    bias_second,
    router,
    router_first,
    router_second,
    norm_gains,
    gains_first,
    gains_second,
    expert_in,
    in_first,
    in_second,
    expert_out,
    down_first,
    down_second,
):
    rows, width = tokens.shape
    experts = router.shape[1]
    capacity = (10 * rows + 4 * experts - 1) // (4 * experts)
    exps = lax.axis_size("exp")
    grps = lax.axis_size("grp")
    routes_t = routes.T
    bias_table = rel_bias.T
    (
        both_w, down_w, cot_all, n_all, comb_all, qkv, pb, context_mine, normed_group, wqkv, wout, hidden_one,
        normed_two, router_probs, in_low, down_low,
    ) = forward_call(
        grps, exps, seq_lengths, bias_table, routes_t, tokens, cotangent, norm_gains.T, router.T,
        attn_qkv, attn_out, expert_in[0], expert_out[0],
    )
    n_total, y_half, y_far, c_in, both_g, down_g, in_before, down_before = expert_call(
        grps, exps, capacity, deal, routes_t, comb_all, n_all, cot_all, both_w, down_w, in_low, down_low,
        hidden_one,
    )
    token_grad, block_out, in_parts, down_parts, qkv_grad, out_grad, small = backward_call(
        grps, exps, seq_lengths, deal, y_half, y_far, both_g, down_g,
        in_before, down_before, normed_group, cot_all, routes_t, tokens, n_total, c_in, normed_two, router_probs, hidden_one, qkv, pb, context_mine, wqkv,
        wout, norm_gains.T, router.T,
    )
    states = [
        attn_qkv, qkv_first, qkv_second, attn_out, out_first, out_second, bias_table, bias_first.T, bias_second.T,
        router.T, router_first.T, router_second.T, norm_gains.T, gains_first.T, gains_second.T,
        expert_in[0], in_first[0], in_second[0], expert_out[0], down_first[0], down_second[0],
    ]
    new = list(adam_call(exps, in_parts, down_parts, qkv_grad, out_grad, small, states))
    new = new[:6] + [array.T for array in new[6:15]] + [array[None] for array in new[15:]]
    return (block_out, token_grad, *new)


def bucket_onehot(length):
    places = jnp.arange(length, dtype=jnp.int32)
    offset = places[None, :] - places[:, None]
    distance = jnp.abs(offset)
    bucket = 16 * (offset > 0).astype(jnp.int32)
    for threshold in thresholds:
        bucket = bucket + (distance >= threshold).astype(jnp.int32)
    return (bucket[:, :, None] == jnp.arange(BUCKETS, dtype=jnp.int32)[None, None, :]).astype(full)


def swap(pieces, axes):
    return lax.all_to_all(pieces, axes, split_axis=0, concat_axis=0, tiled=True)


def spread(block, axes):
    members = lax.axis_size(axes)
    return swap(jnp.broadcast_to(block[None], (members,) + block.shape), axes)


def plain_device(
    tokens,
    cotangent,
    seq_lengths,
    deal,
    routes,
    attn_qkv,
    qkv_first,
    qkv_second,
    attn_out,
    out_first,
    out_second,
    rel_bias,
    bias_first,
    bias_second,
    router,
    router_first,
    router_second,
    norm_gains,
    gains_first,
    gains_second,
    expert_in,
    in_first,
    in_second,
    expert_out,
    down_first,
    down_second,
):
    rows, width = tokens.shape
    head_dim = width // HEADS
    score_scale = 1.0 / math.sqrt(head_dim)
    experts = router.shape[1]
    capacity = (10 * rows + 4 * experts - 1) // (4 * experts)
    exps = lax.axis_size("exp")
    grps = lax.axis_size("grp")
    reps = grps * QUAD
    heads = HEADS // exps
    head_cols = heads * head_dim
    place = lax.axis_index("exp")
    base = lax.axis_index(REP) * exps
    me = base + place
    slab = expert_in.shape[1]
    units = expert_out.shape[1]
    quarter = grps * units

    row_block = attn_qkv.shape[0]
    qkv_rows = lax.all_gather(attn_qkv.astype(low), REP, axis=1, tiled=True)
    out_rows = lax.all_gather(attn_out.astype(low), REP, axis=1, tiled=True)
    qkv_pieces = jnp.transpose(
        qkv_rows.reshape(row_block, 3, exps, head_cols), (2, 0, 1, 3)
    ).reshape(exps, row_block, 3 * head_cols)
    qkv_mine = swap(qkv_pieces, "exp").reshape(width, 3 * head_cols)
    full_out = spread(out_rows, "exp").reshape(width, width)

    group_tokens = spread(tokens, "exp")
    group_cotangent = spread(cotangent, "exp")
    my_cotangent = lax.dynamic_index_in_dim(group_cotangent, deal[me] - base, 0, keepdims=False)

    my_routes = lax.dynamic_slice_in_dim(routes, me * rows, rows, 0)
    places = jnp.arange(rows, dtype=jnp.int32)
    valid_rows = (places < seq_lengths[me]).astype(full)
    group_lengths = lax.dynamic_slice_in_dim(seq_lengths, base, exps, 0)
    key_ok = places[None, :] < group_lengths[:, None]
    gain_one = norm_gains[:, 0]
    gain_two = norm_gains[:, 1]

    chosen = (my_routes[:, :, None] == jnp.arange(experts, dtype=jnp.int32)[None, None, :]).astype(full)
    flat_routes = my_routes.reshape(-1)
    route_hot = (flat_routes[:, None] == jnp.arange(experts, dtype=jnp.int32)[None, :]).astype(jnp.int32)
    before = jnp.cumsum(route_hot, axis=0) - route_hot
    slot_index = jnp.sum(before * route_hot, axis=-1)
    target = (flat_routes * capacity + slot_index).reshape(rows, 2)
    slots = experts * capacity
    slot_ids = jnp.arange(slots, dtype=jnp.int32)
    place_first = slot_ids[:, None] == target[None, :, 0]
    place_second = slot_ids[:, None] == target[None, :, 1]
    place_any = jnp.logical_or(place_first, place_second).astype(low)

    shard_in = expert_in[0].astype(low).reshape(slab, 2, grps, QUAD, units)
    in_pieces = jnp.transpose(shard_in, (1, 3, 0, 2, 4)).reshape(2, 1, QUAD, slab, quarter)
    in_pieces = jnp.broadcast_to(in_pieces, (2, grps, QUAD, slab, quarter)).reshape(
        2, reps, slab, quarter
    )
    down_mine = spread(expert_out[0].astype(low), "grp").reshape(quarter, width)
    gate_mine = swap(in_pieces[0], REP).reshape(width, quarter)
    up_mine = swap(in_pieces[1], REP).reshape(width, quarter)

    upstream = my_cotangent.astype(full) * valid_rows[:, None]

    def to_experts(block):
        sent = block.reshape((1, experts) + block.shape[1:])
        sent = jnp.broadcast_to(sent, (QUAD,) + sent.shape[1:])
        return swap(sent.reshape((QUAD * experts,) + block.shape[1:]), PLANE)

    def dispatch(values):
        return dot(place_any, values).astype(low).reshape(experts, capacity, width)

    expert_upstream = to_experts(dispatch(upstream.astype(low))).reshape(-1, width)
    active_grad_bare = lax.dot_general(
        expert_upstream, down_mine, (((1,), (1,)), ((), ())), preferred_element_type=full
    )

    x_group = group_tokens.astype(full)
    scale_group = lax.rsqrt(jnp.mean(x_group * x_group, axis=-1, keepdims=True) + eps_norm)
    normed_group = (x_group * scale_group * gain_one).astype(low).reshape(exps * rows, width)
    qkv = dot(normed_group, qkv_mine).astype(low).reshape(exps, rows, 3, heads, head_dim)
    queries = qkv[:, :, 0]
    key_rows = qkv[:, :, 1]
    values = qkv[:, :, 2]
    onehot = bucket_onehot(rows)
    bias_mine = lax.dynamic_slice_in_dim(rel_bias, place * heads, heads, 1)
    bias_table = jnp.einsum("ijb,bh->hij", onehot, bias_mine, precision=highest)

    def scores_of():
        raw = (
            jnp.einsum("sihd,sjhd->shij", queries, key_rows, preferred_element_type=full)
            * score_scale
            + bias_table[None]
        )
        return jnp.where(key_ok[:, None, None, :], raw, -1e30)

    scores = scores_of()
    row_max = jnp.max(scores, axis=-1, keepdims=True)
    log_total = row_max + jnp.log(jnp.sum(jnp.exp(scores - row_max), axis=-1, keepdims=True))
    weights_low = jnp.exp(scores - log_total).astype(low)
    context_mine = (
        jnp.einsum("shij,sjhd->sihd", weights_low, values, preferred_element_type=full)
        .astype(low)
        .reshape(exps, rows, head_cols)
    )
    context = jnp.transpose(swap(context_mine, "exp"), (1, 0, 2)).reshape(rows, width)

    x_float = tokens.astype(full)
    scale_one = lax.rsqrt(jnp.mean(x_float * x_float, axis=-1, keepdims=True) + eps_norm)
    hidden_one = x_float + dot(context, full_out)
    scale_two = lax.rsqrt(jnp.mean(hidden_one * hidden_one, axis=-1, keepdims=True) + eps_norm)
    normed_two = (hidden_one * scale_two * gain_two).astype(low)
    normed_float = normed_two.astype(full)
    router_probs = jax.nn.softmax(jnp.dot(normed_float, router, precision=highest), axis=-1)
    picked = jnp.sum(router_probs[:, None, :] * chosen, axis=-1)
    gate_total = jnp.sum(picked, axis=-1, keepdims=True)
    gate_value = picked / gate_total
    combine = gate_value * valid_rows[:, None]
    combine_slots = jnp.sum(
        jnp.where(place_first, combine[None, :, 0], 0.0)
        + jnp.where(place_second, combine[None, :, 1], 0.0),
        axis=1,
    ).reshape(experts, 1, capacity)

    expert_rows = to_experts(dispatch(normed_two)).reshape(-1, width)
    expert_combine = to_experts(combine_slots).reshape(-1, 1)

    gate_part = dot(expert_rows, gate_mine)
    up_part = dot(expert_rows, up_mine)
    active_float, active_pull = jax.vjp(gated_unit, gate_part, up_part)
    active = active_float.astype(low)
    active_scaled = (active_float * expert_combine).astype(low)
    combine_grad_part = jnp.sum(active_float * active_grad_bare, axis=-1).reshape(
        QUAD * experts, 1, capacity
    )
    gate_part_grad, up_part_grad = active_pull(active_grad_bare * expert_combine)
    gate_part_grad = gate_part_grad.astype(low)
    up_part_grad = up_part_grad.astype(low)
    rows_grad_part = (
        lax.dot_general(gate_part_grad, gate_mine, (((1,), (1,)), ((), ())), preferred_element_type=full)
        + lax.dot_general(up_part_grad, up_mine, (((1,), (1,)), ((), ())), preferred_element_type=full)
    ).astype(low)
    output_part = dot(active, down_mine).astype(low)

    combine_grad_back = swap(combine_grad_part, PLANE)
    rows_grad_back = swap(rows_grad_part.reshape(QUAD * experts, capacity, width), PLANE)
    output_back = swap(output_part.reshape(QUAD * experts, capacity, width), PLANE)

    def transposed_dot(a, b):
        return lax.dot_general(a, b, (((0,), (0,)), ((), ())), preferred_element_type=full)

    down_grad = transposed_dot(active_scaled, expert_upstream).astype(low)
    gate_grad = transposed_dot(expert_rows, gate_part_grad).astype(low)
    up_grad = transposed_dot(expert_rows, up_part_grad).astype(low)
    down_share = jnp.sum(
        swap(down_grad.reshape(grps, units, width), "grp").astype(full), axis=0
    )[None]

    def in_columns(grad):
        back = swap(grad.reshape(reps, slab, quarter), REP).astype(full)
        back = jnp.sum(back.reshape(grps, QUAD, slab, grps, units), axis=0)
        return jnp.transpose(back, (1, 2, 0, 3)).reshape(slab, grps * QUAD * units)

    in_share = jnp.concatenate([in_columns(gate_grad), in_columns(up_grad)], axis=1)[None]

    def from_slots(placed, parts):
        hot = jnp.broadcast_to(placed.astype(low)[None], (QUAD,) + placed.shape).reshape(-1, rows)
        return lax.dot_general(
            hot, parts.reshape(-1, width), (((0,), (0,)), ((), ())), preferred_element_type=full
        )

    mixture = combine[:, :1] * from_slots(place_first, output_back) + combine[:, 1:] * from_slots(
        place_second, output_back
    )
    block_loader = (valid_rows[:, None] * (hidden_one + mixture)).astype(low)
    seq_ids = jnp.arange(deal.shape[0], dtype=jnp.int32)
    dealt_seq = jnp.sum(jnp.where(deal == me, seq_ids, 0))
    block_out = lax.dynamic_index_in_dim(
        spread(block_loader, "exp"), dealt_seq - base, 0, keepdims=False
    )

    combine_grad_slots = jnp.sum(combine_grad_back.reshape(QUAD, slots), axis=0)
    combine_grad = jnp.stack(
        [
            jnp.sum(jnp.where(place_first, combine_grad_slots[:, None], 0.0), axis=0),
            jnp.sum(jnp.where(place_second, combine_grad_slots[:, None], 0.0), axis=0),
        ],
        axis=1,
    )
    gate_grad_value = combine_grad * valid_rows[:, None]
    picked_grad = (
        gate_grad_value - jnp.sum(gate_grad_value * gate_value, axis=-1, keepdims=True)
    ) / gate_total
    probs_grad = jnp.sum(picked_grad[:, :, None] * chosen, axis=1)
    logit_grad = router_probs * (
        probs_grad - jnp.sum(probs_grad * router_probs, axis=-1, keepdims=True)
    )
    router_grad = jnp.dot(normed_float.T, logit_grad, precision=highest)
    normed_grad = jnp.dot(logit_grad, router.T, precision=highest) + from_slots(
        jnp.logical_or(place_first, place_second), rows_grad_back
    )
    scaled_two = normed_grad * gain_two
    hidden_grad = (
        upstream
        + scale_two * scaled_two
        - hidden_one * scale_two**3 * jnp.mean(scaled_two * hidden_one, axis=-1, keepdims=True)
    )
    gain_two_grad = jnp.sum(normed_grad * hidden_one * scale_two, axis=0)
    branch_grad = hidden_grad.astype(low)
    context_grad = lax.dot_general(
        branch_grad, full_out, (((1,), (1,)), ((), ())), preferred_element_type=full
    ).astype(low)
    context_grad_pieces = jnp.transpose(context_grad.reshape(rows, exps, head_cols), (1, 0, 2))
    context_grad_mine = swap(context_grad_pieces, "exp").reshape(exps, rows, heads, head_dim)
    branch_group = spread(branch_grad, "exp").reshape(exps * rows, width)
    out_grad = transposed_dot(context_mine.reshape(exps * rows, head_cols), branch_group).astype(low)

    scores = scores_of()
    probs_again = jnp.exp(scores - log_total)
    weights_again = probs_again.astype(low)
    values_grad = jnp.einsum(
        "shij,sihd->sjhd", weights_again, context_grad_mine, preferred_element_type=full
    )
    probs_grad_att = jnp.einsum(
        "sihd,sjhd->shij", context_grad_mine, values, preferred_element_type=full
    )
    row_delta = jnp.sum(probs_grad_att * probs_again, axis=-1, keepdims=True)
    scores_grad = (probs_again * (probs_grad_att - row_delta)).astype(low)
    scores_grad_sum = jnp.sum(scores_grad.astype(full), axis=0)
    bias_grad_mine = jnp.einsum("hij,ijb->bh", scores_grad_sum, onehot, precision=highest)
    bias_grad = lax.dynamic_update_slice_in_dim(
        jnp.zeros((BUCKETS, HEADS), full), bias_grad_mine, place * heads, 1
    )
    queries_grad = (
        jnp.einsum("shij,sjhd->sihd", scores_grad, key_rows, preferred_element_type=full)
        * score_scale
    )
    keys_grad = (
        jnp.einsum("shij,sihd->sjhd", scores_grad, queries, preferred_element_type=full)
        * score_scale
    )
    qkv_grad = (
        jnp.stack([queries_grad, keys_grad, values_grad], axis=2)
        .astype(low)
        .reshape(exps * rows, 3 * head_cols)
    )
    normed_one_part = lax.dot_general(
        qkv_grad, qkv_mine, (((1,), (1,)), ((), ())), preferred_element_type=full
    ).astype(low)
    normed_one_grad = jnp.sum(
        swap(normed_one_part.reshape(exps, rows, width), "exp").astype(full), axis=0
    )
    scaled_one = normed_one_grad * gain_one
    token_grad = (
        hidden_grad
        + scale_one * scaled_one
        - x_float * scale_one**3 * jnp.mean(scaled_one * x_float, axis=-1, keepdims=True)
    )
    gain_one_grad = jnp.sum(normed_one_grad * x_float * scale_one, axis=0)

    qkv_weight_grad = transposed_dot(normed_group, qkv_grad).astype(low)
    qkv_grad_rows = swap(qkv_weight_grad.reshape(exps, row_block, 3 * head_cols), "exp")
    qkv_grad_rows = jnp.transpose(
        qkv_grad_rows.reshape(exps, row_block, 3, head_cols), (1, 2, 0, 3)
    ).reshape(row_block, reps, -1)
    qkv_share = jnp.sum(
        swap(jnp.transpose(qkv_grad_rows, (1, 0, 2)), REP).astype(full), axis=0
    )
    out_pieces = jnp.transpose(out_grad.reshape(row_block, reps, -1), (1, 0, 2))
    out_share = jnp.sum(swap(out_pieces, REP).astype(full), axis=0)

    small = jnp.concatenate(
        [
            router_grad.reshape(-1),
            jnp.stack([gain_one_grad, gain_two_grad], axis=1).reshape(-1),
            bias_grad.reshape(-1),
        ]
    ).reshape(-1, 128)
    small_total = jnp.sum(lax.all_gather(small, ALL, axis=0, tiled=False), axis=0).reshape(-1)
    router_total = small_total[: router.size].reshape(router.shape)
    gains_total = small_total[router.size : router.size + norm_gains.size].reshape(norm_gains.shape)
    bias_total = small_total[router.size + norm_gains.size :].reshape(rel_bias.shape)

    qkv_new = adamw_update(attn_qkv, qkv_first, qkv_second, qkv_share, 1.5 / math.sqrt(D), 0.1)
    out_new = adamw_update(attn_out, out_first, out_second, out_share, 6.0 / math.sqrt(D), 0.1)
    bias_new = adamw_update(rel_bias, bias_first, bias_second, bias_total, 0.3, 0.0)
    router_new = adamw_update(
        router, router_first, router_second, router_total, 1.0 / math.sqrt(D), 0.1
    )
    gains_new = adamw_update(norm_gains, gains_first, gains_second, gains_total, 0.5, 0.0)
    in_new = adamw_update(expert_in, in_first, in_second, in_share, 1.5 / math.sqrt(D), 0.1)
    down_new = adamw_update(
        expert_out, down_first, down_second, down_share, 1.5 / math.sqrt(FF), 0.1
    )
    return (
        (block_out, token_grad)
        + qkv_new
        + out_new
        + bias_new
        + router_new
        + gains_new
        + in_new
        + down_new
    )


def solution(mesh):
    reps, exps = mesh.devices.shape
    split = Mesh(mesh.devices.reshape(reps // QUAD, QUAD, exps), ALL)
    by_rows = P(ALL, None)
    attn = P("exp", REP)
    expert = P("exp", REP, None)
    return jax.shard_map(
        per_device if (reps, exps) == (2 * QUAD, 4) else plain_device,
        mesh=split,
        in_specs=(by_rows, by_rows) + (P(),) * 3 + (attn,) * 6 + (P(),) * 9 + (expert,) * 6,
        out_specs=(by_rows, by_rows) + (attn,) * 6 + (P(),) * 9 + (expert,) * 6,
        check_vma=False,
    )
```

```python
import functools
import math

import jax
import jax.numpy as jnp
from jax import lax
from jax.experimental import pallas as pl
from jax.experimental.pallas import tpu as pltpu
from jax.sharding import Mesh
from jax.sharding import PartitionSpec as P

D = 1024
HEADS = 16
FF = 2816
BUCKETS = 32
STEP = 10
QUAD = 4
REP = ("grp", "quad")
PLANE = ("quad", "exp")
ALL = ("grp", "quad", "exp")

highest = lax.Precision.HIGHEST
eps_norm = 1e-06
thresholds = (1, 2, 3, 4, 5, 6, 7, 8, 11, 16, 22, 32, 45, 64, 90)
beta_one = 0.9
beta_two = 0.999
eps_adam = 1e-08
low = jnp.bfloat16
full = jnp.float32
MESH = pl.DeviceIdType.MESH


def adamw_update(weight, moment, second, gradient, step_rate, decay_factor):
    new_moment = beta_one * moment + (1.0 - beta_one) * gradient
    new_second = beta_two * second + (1.0 - beta_two) * gradient * gradient
    corrected = new_moment / (1.0 - beta_one**STEP)
    scaled = new_second / (1.0 - beta_two**STEP)
    new_weight = weight - step_rate * (
        corrected / (jnp.sqrt(scaled) + eps_adam) + decay_factor * weight
    )
    return (new_moment, new_second, new_weight)


def gated_unit(gate_input, up_input):
    return jax.nn.gelu(gate_input, approximate=True) * up_input


def dot(a, b):
    return jnp.dot(a, b, preferred_element_type=full)


def nt(a, b, precision=None):
    return lax.dot_general(a, b, (((1,), (1,)), ((), ())), preferred_element_type=full, precision=precision)


def tn(a, b):
    return lax.dot_general(a, b, (((0,), (0,)), ((), ())), preferred_element_type=full)


class Where:
    def __init__(self, grps, exps):
        self.grps, self.exps = grps, exps
        self.reps = grps * QUAD
        self.grp = lax.axis_index("grp")
        self.quad = lax.axis_index("quad")
        self.exp = lax.axis_index("exp")
        self.rep = self.grp * QUAD + self.quad
        self.base = self.rep * exps
        self.me = self.base + self.exp

    def device(self, rep, exp):
        return (rep // QUAD, rep % QUAD, exp)

    def near(self, flip):
        q = self.quad
        if flip & 1:
            q = q + 1 - 2 * (q % 2)
        if flip & 2:
            q = q + 2 - 4 * (q // 2)
        return q


def send(src, dst, send_sem, recv_sem, device):
    return pltpu.make_async_remote_copy(
        src_ref=src, dst_ref=dst, send_sem=send_sem, recv_sem=recv_sem, device_id=device, device_id_type=MESH
    )


def arrived(ref, sem):
    pltpu.make_async_copy(ref, ref, sem).wait()


def greet(count, device):
    barrier = pltpu.get_barrier_semaphore()

    def one(k, _):
        pl.semaphore_signal(barrier, inc=1, device_id=device(k), device_id_type=MESH)
        return 0

    lax.fori_loop(1, count + 1, one, 0)
    return functools.partial(pl.semaphore_wait, barrier, count)


def everyone(at):
    count = at.reps * at.exps

    def device(k):
        other = (at.me + k) % count
        return at.device(other // at.exps, other % at.exps)

    return count - 1, device


def neighbours(at):
    members = QUAD * at.exps
    plane = at.quad * at.exps + at.exp

    def device(k):
        other = (plane + k) % members
        rest = k - members
        grp = jnp.where(k < members, at.grp, (at.grp + 1 + rest // QUAD) % at.grps)
        quad = jnp.where(k < members, other // at.exps, rest % QUAD)
        return grp, quad, jnp.where(k < members, other % at.exps, at.exp)

    return members - 1 + QUAD * (at.grps - 1), device


def turn(exp, i):
    beside = exp + 1 - 2 * (exp % 2)
    return jnp.where(i == 0, (beside + 2) % 4, jnp.where(i == 1, (exp + 2) % 4, jnp.where(i == 2, beside, exp)))


def lane_of(shape):
    return lax.broadcasted_iota(jnp.int32, shape, 1)


def row_of(shape):
    return lax.broadcasted_iota(jnp.int32, shape, 0)


def bucket_of(offset):
    distance = jnp.abs(offset)
    bucket = jnp.where(offset > 0, 16, 0)
    for threshold in thresholds:
        bucket = bucket + jnp.where(distance >= threshold, 1, 0)
    return bucket


def bits_of(count):
    return count.bit_length() - 1


def column_parts(width):
    tiles = width // 128
    cuts = [0, (tiles + 2) // 3, (2 * tiles + 2) // 3, tiles]
    return [(cuts[i] * 128, (cuts[i + 1] - cuts[i]) * 128) for i in range(3)]


def flipped(place, bit):
    return place + (1 - 2 * ((place // (1 << bit)) % 2)) * (1 << bit)


class Doubling:
    def __init__(self, at, own, every, sems, core_sems, orders):
        self.at, self.own, self.every = at, own, every
        self.sems, self.core_sems, self.orders = sems, core_sems, orders
        self.plane = at.quad * at.exps + at.exp
        self.steps = len(orders[0])
        self.parts = column_parts(own.shape[1])

    def device(self, bit):
        other = flipped(self.plane, bit)
        return (self.at.grp, other // self.at.exps, other % self.at.exps)

    def place(self, part, j):
        p = self.plane
        for i, bit in enumerate(self.orders[part]):
            if (j >> i) & 1:
                p = flipped(p, bit + 1)
        return p

    def block(self, part, p):
        begin, size = self.parts[part]
        return self.every.at[p, :, pl.ds(begin, size)]

    def source(self, part, j):
        begin, size = self.parts[part]
        return self.own.at[:, pl.ds(begin, size)] if j == 0 else self.block(part, self.place(part, j))

    def index(self, step, part, j):
        return part * (1 << self.steps) + (1 << step) - 1 + j

    def copy(self, step, part, j):
        i = self.index(step, part, j)
        return send(
            self.source(part, j),
            self.block(part, self.place(part, j)),
            self.sems.at[0, i],
            self.sems.at[1, i],
            self.device(self.orders[part][step] + 1),
        )

    def core_copy(self, part, j):
        i = part * (1 << self.steps) + j
        return send(
            self.source(part, j),
            self.block(part, self.place(part, j)),
            self.core_sems.at[0, i],
            self.core_sems.at[1, i],
            self.device(0),
        )

    def start(self):
        for part in range(3):
            for step in range(self.steps):
                self.copy(step, part, 0).start()
        for part in range(3):
            self.core_copy(part, 0).start()
        self.keep().start()

    def keep(self):
        return pltpu.make_async_copy(self.own, self.every.at[self.plane], self.core_sems.at[1, 3 << self.steps])

    def next(self, step):
        for part in range(3):
            for j in range(1 << step):
                k = (1 << step) + j
                arrived(self.block(part, self.place(part, k)), self.sems.at[1, self.index(step, part, j)])
                for later in range(step + 1, self.steps):
                    self.copy(later, part, k).start()
                self.core_copy(part, k).start()

    def finish_in(self):
        for part in range(3):
            for j in range(1 << self.steps):
                there = self.block(part, flipped(self.place(part, j), 0))
                arrived(there, self.core_sems.at[1, part * (1 << self.steps) + j])
        self.keep().wait()

    def finish_out(self):
        for part in range(3):
            for j in range(1 << self.steps):
                self.core_copy(part, j).wait_send()
            for step in range(self.steps):
                for j in range(1 << step):
                    self.copy(step, part, j).wait_send()


class Halving:
    def __init__(self, at, bufs, sems, orders):
        self.at, self.bufs, self.sems = at, bufs, sems
        self.plane = at.quad * at.exps + at.exp
        self.places = bits_of(QUAD * at.exps)
        self.chip_bits = list(range(self.places - 1))
        self.parts = column_parts(bufs[0].shape[2])
        self.orders = orders

    def device(self, bit):
        other = flipped(self.plane, bit)
        return (self.at.grp, other // self.at.exps, other % self.at.exps)

    def hop(self, step, part):
        order = self.orders[part]
        bit = order[step]
        left = [b for b in self.chip_bits if b not in order[:step]]
        pos = left.index(bit)
        half = 1 << (len(left) - 1)
        mine = (self.plane // (1 << (bit + 1))) % 2
        device = self.device(bit + 1)
        begin, size = self.parts[part]
        cols = pl.ds(begin, size)
        base = self.base(step, part)

        def index(j, value):
            return (j >> pos) * (1 << (pos + 1)) + value * (1 << pos) + j % (1 << pos)

        pairs = []
        for j in range(half):
            copy = functools.partial(
                send,
                self.bufs[step].at[index(j, 1 - mine), :, cols],
                self.bufs[step + 1].at[j, :, cols],
                self.sems.at[0, base + j],
                self.sems.at[1, base + j],
                device,
            )
            pairs.append((copy, index(j, mine), j))
        return pairs, begin, size, base

    def base(self, step, part):
        n = len(self.chip_bits)
        return part * (1 << n) + sum(1 << (n - 1 - s) for s in range(step))

    def start(self, step, part=None):
        for p in range(3) if part is None else [part]:
            for copy, _, _ in self.hop(step, p)[0]:
                copy().start()

    def add(self, step, part):
        pairs, begin, size, base = self.hop(step, part)
        cols = pl.ds(begin, size)
        here, there = self.bufs[step], self.bufs[step + 1]
        for _, keep, j in pairs:
            arrived(there.at[j, :, cols], self.sems.at[1, base + j])
            there[j, :, begin : begin + size] = (
                there[j, :, begin : begin + size] + here[keep, :, begin : begin + size]
            )

    def next(self, step):
        for p in range(3):
            self.add(step, p)
            if step + 1 < len(self.chip_bits):
                self.start(step + 1, p)

    def result(self):
        return self.bufs[len(self.chip_bits)]

    def finish(self):
        for step in range(len(self.chip_bits)):
            for p in range(3):
                for copy, _, _ in self.hop(step, p)[0]:
                    copy().wait_send()


class Group:
    def __init__(self, at, own, every, sems):
        self.at, self.own, self.every, self.sems = at, own, every, sems
        self.beside, self.across = at.exp + 1 - 2 * (at.exp % 2), (at.exp + 2) % 4

    def copy(self, src, index, send_index, device):
        return send(
            src, self.every.at[index], self.sems.at[0, send_index], self.sems.at[1, index], self.at.device(self.at.rep, device)
        )

    def first(self):
        return [
            self.copy(self.own, self.at.exp, 0, self.across),
            self.copy(self.own, self.at.exp, 1, self.beside),
        ]

    def second(self):
        return self.copy(self.every.at[self.across], self.across, 2, self.beside)

    def start(self):
        for copy in self.first():
            copy.start()

    def pass_on(self):
        arrived(self.every.at[self.across], self.sems.at[1, self.across])
        self.second().start()

    def arrive(self):
        for index in (self.beside, (self.beside + 2) % 4):
            arrived(self.every.at[index], self.sems.at[1, index])

    def sent(self):
        for copy in self.first() + [self.second()]:
            copy.wait_send()


class Tiles:
    def __init__(self, units, reps):
        self.units = units
        self.reps = reps
        self.hidden = units * reps
        self.half = self.hidden // 256
        self.wide = (self.half + 1) // 2
        self.count = 3
        self.size = 128 * self.wide // self.count
        self.skip = 128 * (2 * self.wide - self.half)

    def start(self, quad):
        return 128 * (self.half * (quad // 2) + (self.half - self.wide) * (quad % 2))

    def rows(self, tile):
        result = []
        for k in range(QUAD):
            found = None
            for parity in range(2):
                first = self.start(parity) + tile * self.size
                live = first + (self.skip if parity and tile == 0 else 0)
                begin = max(live, k * self.units)
                end = min(first + self.size, (k + 1) * self.units)
                if end > begin:
                    found = (begin - k * self.units, end - begin, parity, begin - first)
            result.append(found)
        return result


class Outward:
    def __init__(self, at, tiles, tile, in_low, down_slab, both_w, down_w, nothing, sems, down_sems):
        self.at, self.tiles, self.tile = at, tiles, tile
        self.in_low, self.down_slab, self.both_w, self.down_w = in_low, down_slab, both_w, down_w
        self.nothing, self.sems, self.down_sems = nothing, sems, down_sems
        self.slab = in_low.shape[0]

    def source(self, quad, section):
        begin = section * self.tiles.hidden + self.tiles.start(quad) + self.tile * self.tiles.size
        return self.in_low.at[:, pl.ds(pl.multiple_of(begin, 128), self.tiles.size)]

    def target(self, rep, section):
        rows = pl.ds(pl.multiple_of(rep * self.slab, self.slab), self.slab)
        return self.both_w.at[rows, pl.ds(section * self.tiles.size, self.tiles.size)]

    def over(self, act, first=1, last=None):
        at = self.at

        def one(k, _):
            other = (at.rep + k) % at.reps
            for section in range(2):
                act(
                    functools.partial(
                        send,
                        self.source(other % QUAD, section),
                        self.target(at.rep, section),
                        self.sems.at[0, section * at.reps + other],
                        self.sems.at[1, section * at.reps + at.rep],
                        at.device(other, at.exp),
                    )
                )
            return 0

        lax.fori_loop(first, last or at.reps, one, 0)

    def over_down(self, act, act_local):
        at = self.at
        for k, piece in enumerate(self.tiles.rows(self.tile)):
            if piece is None:
                continue
            begin, count, parity, to = piece
            quad = 2 * (at.rep // QUAD) + parity
            src, dst = self.down_slab.at[pl.ds(begin, count)], self.down_w.at[pl.ds(to, count)]
            recv = self.down_sems.at[1, at.rep]
            for g in range(at.grps):
                stays = jnp.logical_and(at.grp == g, at.quad == quad)
                ours = at.rep % QUAD == k

                @pl.when(jnp.logical_and(ours, jnp.logical_not(stays)))
                def _():
                    act(functools.partial(send, src, dst, self.down_sems.at[0, g], recv, (g, quad, at.exp)))

                @pl.when(jnp.logical_and(ours, stays))
                def _():
                    act_local(functools.partial(pltpu.make_async_copy, src, dst, recv))

    def blank(self):
        return pltpu.make_async_copy(
            self.nothing, self.down_w.at[pl.ds(0, self.tiles.skip)], self.down_sems.at[1, self.at.reps]
        )

    def start(self, first=1, last=None):
        at = self.at
        self.over(lambda copy: copy().start(), first, last)
        if first > 1:
            return
        self.over_down(lambda copy: copy().start(), lambda copy: copy().start())
        for section in range(2):
            pltpu.make_async_copy(
                self.source(at.quad, section), self.target(at.rep, section), self.sems.at[1, section * at.reps + at.rep]
            ).start()
        if self.tile == 0:

            @pl.when(at.quad % 2 == 1)
            def _():
                self.blank().start()

    def arrive(self):
        at = self.at

        def one(rep, _):
            for section in range(2):
                arrived(self.target(rep, section), self.sems.at[1, section * at.reps + rep])
            return 0

        lax.fori_loop(0, at.reps, one, 0)
        for parity in range(2):

            @pl.when(at.quad % 2 == parity)
            def _():
                for k, piece in enumerate(self.tiles.rows(self.tile)):
                    if piece is not None and piece[2] == parity:
                        source = QUAD * (at.quad // 2) + k
                        arrived(self.down_w.at[pl.ds(piece[3], piece[1])], self.down_sems.at[1, source])
                if parity and self.tile == 0:
                    self.blank().wait()

    def sent(self):
        self.over(lambda copy: copy().wait_send())
        self.over_down(lambda copy: copy().wait_send(), lambda copy: None)


class Homeward:
    def __init__(self, at, tiles, tile, both, down, in_parts, down_parts, sems, down_sems, sections=(0, 1)):
        self.at, self.tiles, self.tile, self.sections = at, tiles, tile, sections
        self.both, self.down, self.in_parts, self.down_parts = both, down, in_parts, down_parts
        self.sems, self.down_sems = sems, down_sems
        self.slab = in_parts.shape[1]

    def target(self, grp, quad, parity, section):
        skip = self.tiles.skip if parity and self.tile == 0 else 0
        to = section * self.tiles.hidden + self.tiles.start(quad) + self.tile * self.tiles.size + skip
        to = to if isinstance(to, int) else pl.multiple_of(to, 128)
        return skip, self.in_parts.at[grp, :, pl.ds(to, self.tiles.size - skip)]

    def copy(self, rep, parity, section, local=False):
        at = self.at
        skip, dst = self.target(at.grp, at.quad, parity, section)
        rows = pl.ds(pl.multiple_of(rep * self.slab, self.slab), self.slab)
        src = self.both.at[rows, pl.ds(section * self.tiles.size + skip, self.tiles.size - skip)]
        recv = self.sems.at[1, section * at.reps + at.rep]
        if local:
            return pltpu.make_async_copy(src, dst, recv)
        return send(src, dst, self.sems.at[0, section * at.reps + rep], recv, at.device(rep, at.exp))

    def over(self, act, act_local):
        at = self.at
        for parity in range(2):

            @pl.when(at.quad % 2 == parity)
            def _():
                def one(k, _):
                    for section in self.sections:
                        act(self.copy((at.rep + k) % at.reps, parity, section))
                    return 0

                lax.fori_loop(1, at.reps, one, 0)
                if act_local:
                    for section in self.sections:
                        act_local(self.copy(at.rep, parity, section, local=True))

    def over_down(self, act, act_local):
        at = self.at
        if self.down is None:
            return
        for k, piece in enumerate(self.tiles.rows(self.tile)):
            if piece is None:
                continue
            begin, count, parity, to = piece
            src, dst = self.down.at[pl.ds(to, count)], self.down_parts.at[at.grp, pl.ds(begin, count)]
            recv = self.down_sems.at[1, at.grp]
            stays = jnp.logical_and(at.grp == at.quad // 2, at.quad == k)
            ours = at.quad % 2 == parity

            @pl.when(jnp.logical_and(ours, jnp.logical_not(stays)))
            def _():
                act(functools.partial(send, src, dst, self.down_sems.at[0, k], recv, (at.quad // 2, k, at.exp)))

            @pl.when(jnp.logical_and(ours, stays))
            def _():
                act_local(functools.partial(pltpu.make_async_copy, src, dst, recv))

    def start(self):
        self.over_down(lambda copy: copy().start(), lambda copy: copy().start())
        self.over(lambda copy: copy.start(), lambda copy: copy.start())

    def arrive(self):
        at = self.at
        for rep in range(at.reps):
            for section in self.sections:
                _, dst = self.target(rep // QUAD, rep % QUAD, rep % 2, section)
                arrived(dst, self.sems.at[1, section * at.reps + rep])
        for k, piece in enumerate(self.tiles.rows(self.tile)):
            if piece is None or self.down is None:
                continue

            @pl.when(at.quad == k)
            def _():
                for g in range(at.grps):
                    arrived(self.down_parts.at[g, pl.ds(piece[0], piece[1])], self.down_sems.at[1, g])

    def sent(self):
        self.over(lambda copy: copy.wait_send(), None)
        self.over_down(lambda copy: copy().wait_send(), lambda copy: None)


def forward_kernel(
    grps,
    exps,
    lengths,
    bias_table,
    routes_t,
    tokens,
    cotangent,
    gains,
    router,
    attn_qkv,
    attn_out,
    expert_in,
    expert_out,
    both_w,
    down_w,
    cot_all,
    n_all,
    comb_all,
    qkv_out,
    pb_out,
    mine_out,
    n1_out,
    wqkv_out,
    wout_out,
    h1_out,
    n2_out,
    probs_out,
    in_out,
    down_out,
    in_wide,
    down_wide,
    qkv_t,
    out_w,
    in_low,
    down_slab,
    tok_all,
    wqkv,
    wout,
    n1,
    qkv,
    pb,
    mine,
    ctx,
    bias,
    comb_send,
    nothing,
    tok_sem,
    wq_sem,
    wo_sem,
    wo2_sem,
    weight_sem,
    down_sem,
    ctx_sem,
    cot_sem,
    cot_core_sem,
    n_sem,
    n_core_sem,
    comb_sem,
    store_sem,
    cast_sem,
):
    at = Where(grps, exps)
    reps = at.reps
    rows, width = tokens.shape
    heads = HEADS // exps
    head_dim = width // HEADS
    head_cols = heads * head_dim
    block_cols = min(128, head_cols)
    shard_cols, row_block = qkv_t.shape
    seg = math.gcd(shard_cols, head_cols)
    segs = shard_cols // seg
    tiles = Tiles(down_slab.shape[0], reps)
    plane = at.quad * exps + at.exp
    members = QUAD * exps
    scale = 1.0 / math.sqrt(head_dim)
    SEND, RECV = 0, 1

    met = greet(*everyone(at))
    wide_copies = [
        pltpu.make_async_copy(expert_in, in_wide, cast_sem.at[0]),
        pltpu.make_async_copy(expert_out, down_wide, cast_sem.at[1]),
    ]
    for copy in wide_copies:
        copy.start()
    qkv_t[...] = attn_qkv[...].T.astype(low)
    out_w[...] = attn_out[...].astype(low)
    met()

    def exp_peer(k):
        return (at.exp + k) % exps

    group_tokens = Group(at, tokens, tok_all, tok_sem)
    group_tokens.start()
    tok_all[at.exp] = tokens[...]

    def segment(k):
        col = (at.rep * segs + k) * seg
        section = col // width
        within = col - section * width
        owner = within // head_cols
        return owner, section * head_cols + within - owner * head_cols

    def segment_copy(k, shift):
        owner, offset = segment(k)
        src = qkv_t.at[pl.ds(k * seg, seg)]
        dst = wqkv.at[at.exp, pl.ds(pl.multiple_of(offset, seg), seg)]
        target = at.device((at.rep + shift) % reps, owner)
        return owner, src, dst, functools.partial(
            send, src, dst, wq_sem.at[SEND, k * reps + shift], wq_sem.at[RECV, at.exp * 3 * (head_cols // seg) + offset // seg], target
        )

    def over_segments(act, act_local):
        def one(i, _):
            k, shift = i // reps, i % reps
            owner, src, dst, copy = segment_copy(k, shift)
            stays = jnp.logical_and(shift == 0, owner == at.exp)

            @pl.when(jnp.logical_not(stays))
            def _():
                act(copy())

            @pl.when(stays)
            def _():
                act_local(k, src, dst)

            return 0

        lax.fori_loop(0, segs * reps, one, 0)

    def local_segment(k, src, dst):
        _, offset = segment(k)
        pltpu.make_async_copy(src, dst, wq_sem.at[RECV, at.exp * 3 * (head_cols // seg) + offset // seg]).start()

    over_segments(lambda copy: copy.start(), local_segment)

    for k in range(1, reps):
        other = (at.rep + k) % reps
        send(
            out_w, wout.at[at.exp, at.rep], wo_sem.at[SEND, other], wo_sem.at[RECV, at.rep], at.device(other, at.exp)
        ).start()
    wout[at.exp, at.rep] = out_w[...]
    chip_bits = list(range(bits_of(members) - 1))
    cots = Doubling(at, cotangent, cot_all, cot_sem, cot_core_sem, [chip_bits[::-1]] * 3)
    cots.start()

    span = 2 * rows
    bucket = bucket_of(lane_of((8, span)) - rows)
    for h in range(heads):
        line = jnp.zeros((8, span), full)
        for b in range(BUCKETS):
            line = jnp.where(bucket == b, bias_table[at.exp * heads + h, b], line)
        whole = jnp.broadcast_to(line[0:1], (rows, span))
        bias[h] = pltpu.roll(whole, 0, 1, stride=1, stride_axis=0)[:, rows:]

    group_tokens.pass_on()
    group_tokens.arrive()

    def norm_group(s, _):
        x = tok_all[s].astype(full)
        r = lax.rsqrt(jnp.mean(x * x, axis=1, keepdims=True) + eps_norm)
        n1[s] = (x * r * gains[0:1, :]).astype(low)
        return 0

    lax.fori_loop(0, exps, norm_group, 0)

    for copy in wide_copies:
        copy.wait()
    in_low[...] = in_wide[...].astype(low)
    down_slab[...] = down_wide[...].astype(low)
    nothing[...] = jnp.zeros_like(nothing)
    weights = [
        Outward(
            at, tiles, t, in_low, down_slab, both_w.at[t], down_w.at[t], nothing, weight_sem.at[t], down_sem.at[t]
        )
        for t in range(2)
    ]

    weights[0].start()

    def wait_segment(i, _):
        e, j = i // (3 * head_cols // seg), i % (3 * head_cols // seg)
        arrived(wqkv.at[e, pl.ds(pl.multiple_of(j * seg, seg), seg)], wq_sem.at[RECV, i])
        return 0

    lax.fori_loop(0, exps * 3 * head_cols // seg, wait_segment, 0)

    def project(s, _):
        total = jnp.zeros((rows, 3 * head_cols), full)
        for e in range(exps):
            total = total + nt(n1[s, :, e * row_block : (e + 1) * row_block], wqkv[e])
        qkv[s] = total.astype(low)
        return 0

    lax.fori_loop(0, exps, project, 0)

    group_wout = Group(at, wout.at[at.exp], wout, wo2_sem)

    def beside(k):
        if k == 1:
            for j in range(1, reps):
                other = (at.rep + j) % reps
                arrived(wout.at[at.exp, other], wo_sem.at[RECV, other])
            group_wout.start()
        elif k == 2:
            cots.next(0)
        else:
            group_wout.pass_on()

    def attend(i, _):
        s = turn(at.exp, i)
        for k in range(1, exps):

            @pl.when(i == k)
            def _():
                beside(k)

        ok = lane_of((rows, rows)) < lengths[at.base + s]
        lane = lane_of((rows, block_cols))
        for c in range(head_cols // block_cols):
            cols = slice(c * block_cols, (c + 1) * block_cols)
            q = qkv[s, :, cols] * scale
            k = qkv[s, :, head_cols + c * block_cols : head_cols + (c + 1) * block_cols]
            v = qkv[s, :, 2 * head_cols + c * block_cols : 2 * head_cols + (c + 1) * block_cols]
            result = jnp.zeros((rows, block_cols), full)
            for t in range(block_cols // head_dim):
                h = c * (block_cols // head_dim) + t
                here = jnp.logical_and(lane >= t * head_dim, lane < (t + 1) * head_dim)
                scores = nt(jnp.where(here, q, jnp.zeros_like(q)), k) + bias[h]
                scores = jnp.where(ok, scores, -1e30)
                top = jnp.max(scores, axis=1, keepdims=True)
                weights = jnp.exp(scores - top)
                total = jnp.sum(weights, axis=1, keepdims=True)
                weights = (weights * (1.0 / total)).astype(low)
                result = jnp.where(here, jnp.dot(weights, v, preferred_element_type=full), result)
                pb[s * heads + h] = weights
            mine[s, :, cols] = result.astype(low)

        @pl.when(i < exps - 1)
        def _():
            send(
                mine.at[s], ctx.at[at.exp], ctx_sem.at[SEND, s], ctx_sem.at[RECV, at.exp], at.device(at.rep, s)
            ).start()

        @pl.when(i == exps - 1)
        def _():
            pltpu.make_async_copy(mine.at[s], ctx.at[at.exp], ctx_sem.at[RECV, at.exp]).start()

        return 0

    lax.fori_loop(0, exps, attend, 0)

    cots.next(1)
    group_wout.arrive()
    for e in range(exps):
        arrived(ctx.at[e], ctx_sem.at[RECV, e])

    out_cols = wout.shape[3]
    for r in range(reps):
        cols = slice(r * out_cols, (r + 1) * out_cols)
        total = tokens[:, cols].astype(full)
        for e in range(exps):
            total = total + jnp.dot(ctx[e], wout[e, r], preferred_element_type=full)
        h1_out[:, cols] = total
    h1 = h1_out[...]
    r2 = lax.rsqrt(jnp.mean(h1 * h1, axis=1, keepdims=True) + eps_norm)
    n2 = (h1 * r2 * gains[1:2, :]).astype(low)
    n2_out[...] = n2
    rotated = [chip_bits[c:] + chip_bits[:c] for c in range(3)]
    rows_two = Doubling(at, n2_out, n_all, n_sem, n_core_sem, rotated)
    rows_two.start()
    weights[1].start(1, 3)

    router_rows = jnp.concatenate([router[...], jnp.zeros((128 - exps, width), full)], axis=0)
    logits = nt(n2.astype(full), router_rows, precision=highest)
    lane = lane_of((rows, 128))
    logits = jnp.where(lane < exps, logits, -1e30)
    probs = jnp.exp(logits - jnp.max(logits, axis=1, keepdims=True))
    probs = probs / jnp.sum(probs, axis=1, keepdims=True)
    probs_out[...] = probs
    picked = jnp.where(routed(routes_t, at.me, rows), probs, 0.0)
    comb = picked / jnp.sum(picked, axis=1, keepdims=True)
    comb = jnp.where(row_of((rows, 1)) < lengths[at.me], comb, 0.0)
    comb_send[...] = comb.T[0 : comb_send.shape[0]]

    def comb_copy(k):
        other = (plane + k) % members
        return send(
            comb_send,
            comb_all.at[plane],
            comb_sem.at[SEND, other],
            comb_sem.at[RECV, plane],
            (at.grp, other // exps, other % exps),
        )

    def start_comb(k, _):
        comb_copy(k).start()
        return 0

    lax.fori_loop(1, members, start_comb, 0)
    pltpu.make_async_copy(comb_send, comb_all.at[plane], comb_sem.at[RECV, plane]).start()
    rows_two.next(0)
    weights[1].start(3, 5)

    stores = [
        (qkv, qkv_out),
        (pb, pb_out),
        (mine, mine_out),
        (n1, n1_out),
        (wqkv, wqkv_out),
        (wout, wout_out),
        (in_low, in_out),
        (down_slab, down_out),
    ]
    for i, (src, dst) in enumerate(stores):
        pltpu.make_async_copy(src, dst, store_sem.at[i]).start()

    rows_two.next(1)
    weights[1].start(5)
    for step in range(2, rows_two.steps):
        rows_two.next(step)
    for step in range(2, cots.steps):
        cots.next(step)

    cots.finish_in()
    rows_two.finish_in()

    def comb_in(k, _):
        arrived(comb_all.at[k], comb_sem.at[RECV, k])
        return 0

    lax.fori_loop(0, members, comb_in, 0)
    for tile in weights:
        tile.arrive()

    for k in range(1, exps):
        peer = exp_peer(k)
        arrived(mine.at[peer], ctx_sem.at[SEND, peer])
    over_segments(lambda copy: copy.wait_send(), lambda k, src, dst: None)
    for k in range(1, reps):
        arrived(out_w, wo_sem.at[SEND, (at.rep + k) % reps])
    group_tokens.sent()
    group_wout.sent()
    cots.finish_out()
    rows_two.finish_out()

    def sent_comb(k, _):
        comb_copy(k).wait_send()
        return 0

    lax.fori_loop(1, members, sent_comb, 0)
    for tile in weights:
        tile.sent()
    for i, (src, dst) in enumerate(stores):
        pltpu.make_async_copy(src, dst, store_sem.at[i]).wait()


def forward_call(
    grps, exps, lengths, bias_table, routes_t, tokens, cotangent, gains, router, attn_qkv, attn_out, expert_in, expert_out
):
    reps = grps * QUAD
    rows, width = tokens.shape
    head_cols = width // exps
    row_block, shard_cols = attn_qkv.shape
    seg = math.gcd(shard_cols, head_cols)
    segs = shard_cols // seg
    units = expert_out.shape[0]
    out_cols = attn_out.shape[1]
    heads = HEADS // exps
    members = QUAD * exps
    tiles = Tiles(units, reps)
    shape = jax.ShapeDtypeStruct
    vmem = pl.BlockSpec(memory_space=pltpu.VMEM)
    smem = pl.BlockSpec(memory_space=pltpu.SMEM)
    hbm = pl.BlockSpec(memory_space=pl.ANY)
    results = [
        (shape((2, width, 2 * tiles.size), low), hbm),
        (shape((2, tiles.size, width), low), hbm),
        (shape((members, rows, width), low), hbm),
        (shape((members, rows, width), low), hbm),
        (shape((members, 8, rows), full), hbm),
        (shape((exps, rows, 3 * head_cols), low), hbm),
        (shape((exps * heads, rows, rows), low), hbm),
        (shape((exps, rows, head_cols), low), hbm),
        (shape((exps, rows, width), low), hbm),
        (shape((exps, 3 * head_cols, row_block), low), hbm),
        (shape((exps, reps, row_block, out_cols), low), hbm),
        (shape((rows, width), full), vmem),
        (shape((rows, width), low), vmem),
        (shape((rows, 128), full), vmem),
        (shape(expert_in.shape, low), hbm),
        (shape(expert_out.shape, low), hbm),
    ]
    dma = pltpu.SemaphoreType.DMA
    chips = members // 2
    return pl.pallas_call(
        functools.partial(forward_kernel, grps, exps),
        out_shape=[r[0] for r in results],
        in_specs=[smem] * 2 + [vmem] * 7 + [hbm] * 2,
        out_specs=[r[1] for r in results],
        scratch_shapes=[
            pltpu.VMEM(expert_in.shape, full),
            pltpu.VMEM(expert_out.shape, full),
            pltpu.VMEM((shard_cols, row_block), low),
            pltpu.VMEM((row_block, out_cols), low),
            pltpu.VMEM(expert_in.shape, low),
            pltpu.VMEM(expert_out.shape, low),
            pltpu.VMEM((exps, rows, width), low),
            pltpu.VMEM((exps, 3 * head_cols, row_block), low),
            pltpu.VMEM((exps, reps, row_block, out_cols), low),
            pltpu.VMEM((exps, rows, width), low),
            pltpu.VMEM((exps, rows, 3 * head_cols), low),
            pltpu.VMEM((exps * heads, rows, rows), low),
            pltpu.VMEM((exps, rows, head_cols), low),
            pltpu.VMEM((exps, rows, head_cols), low),
            pltpu.VMEM((heads, rows, rows), full),
            pltpu.VMEM((8, rows), full),
            pltpu.VMEM((tiles.skip, width), low),
            dma((2, exps)),
            dma((2, max(segs * reps, exps * 3 * head_cols // seg))),
            dma((2, reps)),
            dma((2, exps)),
            dma((2, 2, 2 * reps)),
            dma((2, 2, reps + 1)),
            dma((2, exps)),
            dma((2, 3 * chips)),
            dma((2, 3 * chips + 1)),
            dma((2, 3 * chips)),
            dma((2, 3 * chips + 1)),
            dma((2, members)),
            dma((8,)),
            dma((2,)),
        ],
        compiler_params=pltpu.CompilerParams(
            collective_id=0, has_side_effects=True, vmem_limit_bytes=60 * 1024 * 1024
        ),
        name="forward",
    )(lengths, bias_table, routes_t, tokens, cotangent, gains, router, attn_qkv, attn_out, expert_in, expert_out)


def expert_kernel(
    grps,
    exps,
    cap,
    deal,
    routes_t,
    comb,
    n_all,
    cot_all,
    both_w,
    down_w,
    in_low,
    down_slab,
    h1,
    n_total,
    y_half,
    y_far,
    c_in,
    both_g,
    down_g,
    in_parts,
    down_parts,
    place,
    marks,
    n_rows,
    g_rows,
    both_v,
    down_v,
    raw_n,
    raw_g,
    y_acc,
    n_acc,
    both_d,
    active,
    n_bufs,
    c_sum,
    out_y,
    load_sem,
    raw_sem,
    out_sem,
    in_sem,
    in_down_sem,
    home_sem,
    home_down_sem,
    stage_sem,
    far_sem,
    n_sem,
    c_sem,
):
    at = Where(grps, exps)
    rows, width = n_all.shape[1:]
    tiles = Tiles(down_slab.shape[0], at.reps)
    size = tiles.size
    slots = exps * cap
    members = QUAD * exps
    loads = [pltpu.make_async_copy(both_w.at[t], both_v.at[t], load_sem.at[0, t]) for t in range(2)] + [
        pltpu.make_async_copy(down_w.at[t], down_v.at[t], load_sem.at[1, t]) for t in range(2)
    ]
    for copy in loads:
        copy.start()

    def raw_copies(q):
        here = pl.ds(pl.multiple_of(q * exps, exps), exps)
        return [
            pltpu.make_async_copy(n_all.at[here], raw_n.at[pl.ds(q % 2 * exps, exps)], raw_sem.at[0, q % 2]),
            pltpu.make_async_copy(cot_all.at[here], raw_g.at[pl.ds(q % 2 * exps, exps)], raw_sem.at[1, q % 2]),
        ]

    for copy in raw_copies(0):
        copy.start()

    beside = at.exp + 1 - 2 * (at.exp % 2)
    greet(*neighbours(at))()
    last = tiles.count - 1
    incoming = Outward(
        at, tiles, last, in_low, down_slab, both_v.at[last], down_v.at[last], None, in_sem, in_down_sem
    )
    incoming.start()
    home = Homeward(
        at, tiles, 0, both_v.at[0], down_v.at[0], in_parts, down_parts, home_sem, home_down_sem
    )

    earlier = jnp.where(row_of((rows, rows)) < lane_of((rows, rows)), 1.0, 0.0).astype(low)
    slot = row_of((cap, rows)).astype(full)

    def dispatch(q, _):
        @pl.when(q + 1 < QUAD)
        def _():
            for copy in raw_copies(q + 1):
                copy.start()

        for copy in raw_copies(q):
            copy.wait()
        lines = []
        for j in range(exps):
            seq = at.grp * members + q * exps + j
            pair = routes_t[:, pl.ds(pl.multiple_of(seq * rows, rows), rows)]
            lines.append(jnp.logical_or(pair[0:1] == at.exp, pair[1:2] == at.exp))
        lines = [jnp.where(line, 1.0, 0.0) for line in lines] + [jnp.zeros((8 - exps, rows), full)]
        hot_low = jnp.concatenate(lines, axis=0).astype(low)
        before = dot(hot_low, earlier)
        for j in range(exps):
            s = q * exps + j
            inside = jnp.logical_and(slot == before[j : j + 1, :], hot_low[j : j + 1, :].astype(full) > 0.5)
            here = jnp.where(inside, 1.0, 0.0)
            place[s] = here.astype(low)
            g = raw_g[q % 2 * exps]
            for b in range(1, exps):
                g = jnp.where(deal[at.grp * members + s] == at.grp * members + q * exps + b, raw_g[q % 2 * exps + b], g)
            where = pl.ds(pl.multiple_of(s * cap, cap), cap)
            n_rows[where] = dot(here.astype(low), raw_n[q % 2 * exps + j]).astype(low)
            g_rows[where] = dot(here.astype(low), g).astype(low)
            marks[where, 0:1] = jnp.sum(here * comb[s, pl.ds(at.exp, 1), :], axis=1, keepdims=True)
            marks[where, 1:2] = jnp.zeros((cap, 1), full)
        return 0

    lax.fori_loop(0, QUAD, dispatch, 0)
    for copy in loads:
        copy.wait()
    curve = math.sqrt(2.0 / math.pi)

    core = at.exp % 2

    plane = at.quad * exps + at.exp
    sibling = at.device(at.rep, beside)
    dn = Halving(at, n_bufs, n_sem, [[0, 1, 2], [1, 2, 0], [2, 0, 1]])

    def n_copy(j):
        return send(raw_n.at[j], n_bufs[0].at[j], far_sem.at[0, 0, j], far_sem.at[0, 1, j], sibling)

    def y_copies(j):
        return (
            pltpu.make_async_copy(out_y.at[j % 2], y_half.at[j], out_sem.at[j % 2]),
            send(raw_n.at[j], y_far.at[j], far_sem.at[1, 0, j], far_sem.at[1, 1, j], sibling),
        )

    def c_copy(k):
        other = (plane + k) % members
        return send(
            c_sum.at[other],
            c_in.at[plane],
            c_sem.at[0, other],
            c_sem.at[1, plane],
            (at.grp, other // exps, other % exps),
        )

    def slots_of(s):
        return pl.ds(pl.multiple_of(s * cap, cap), cap)

    def n_rows_of(s):
        where = slots_of(s)
        line = jnp.sum(place[s].astype(full) * marks[where, 1:2], axis=0, keepdims=True)
        c_sum[s] = jnp.broadcast_to(line, (8, rows))
        return tn(place[s], n_acc[where]).astype(low)

    def y_rows_of(p):
        first = p // exps * exps
        spot = at.grp * members + p
        here, y = place[first], y_acc[slots_of(first)]
        for c in range(1, exps):
            taken = deal[at.grp * members + first + c] == spot
            here = jnp.where(taken, place[first + c], here)
            y = jnp.where(taken, y_acc[slots_of(first + c)], y)
        return (tn(here, y) + jnp.where(deal[at.me] == spot, h1[...], 0.0)).astype(low)

    def give_n(j):
        raw_n[j] = n_rows_of(2 * j + 1 - core)
        n_copy(j).start()
        raw_g[j] = n_rows_of(2 * j + core)

    def add_n(quad):
        for k in range(exps // 2):
            j = quad * (exps // 2) + k
            arrived(n_bufs[0].at[j], far_sem.at[0, 1, j])
            n_bufs[0][j] = n_bufs[0][j] + raw_g[j]

    def give_y(j, _):
        @pl.when(j >= 2)
        def _():
            y_copies(j - 2)[0].wait()

        out_y[j % 2] = y_rows_of(2 * j + core)
        n_copy(j).wait_send()
        raw_n[j] = y_rows_of(2 * j + 1 - core)
        for copy in y_copies(j):
            copy.start()
        return 0

    def start_c(k, _):
        c_copy(k).start()
        return 0

    def tile_work(f, _):
        @pl.when(f == last)
        def _():
            incoming.arrive()
            home.start()

        def chunk(i, _):
            c = jnp.where(i == 0, at.near(3), jnp.where(i == 1, at.near(1), jnp.where(i == 2, at.near(2), at.quad)))
            here = pl.ds(pl.multiple_of(c * slots, slots), slots)
            share = marks[here, 0:1]
            both = dot(n_rows[here], both_v[f])
            gate_part, up_part = both[:, :size], both[:, size:]
            grad = nt(g_rows[here], down_v[f])
            square = gate_part * gate_part
            bend = jnp.tanh(curve * gate_part * (1.0 + 0.044715 * square))
            half = 0.5 * (1.0 + bend)
            gelu = gate_part * half
            slope = half + (0.5 * curve) * gate_part * (1.0 - bend * bend) * (1.0 + (3 * 0.044715) * square)
            value = gelu * up_part
            marks[here, 1:2] += jnp.sum(value * grad, axis=1, keepdims=True)
            grad = grad * share
            active[f % 2, here] = (value * share).astype(low)
            both_d[f % 2, here, :size] = (grad * up_part * slope).astype(low)
            both_d[f % 2, here, size:] = (grad * gelu).astype(low)
            y = dot(active[f % 2, here], down_v[f])
            y_acc[here] = jnp.where(f == 0, y, y_acc[here].astype(full) + y).astype(low)
            n_back = nt(both_d[f % 2, here], both_v[f])
            n_acc[here] = jnp.where(f == 0, n_back, n_acc[here].astype(full) + n_back).astype(low)

            @pl.when(f == last)
            def _():
                for k in range(exps // 2):
                    give_n(c * (exps // 2) + k)

            @pl.when(jnp.logical_and(f == last, i == 2))
            def _():
                add_n(at.near(3))

            @pl.when(jnp.logical_and(f == last, i == 3))
            def _():
                add_n(at.near(1))
                dn.start(0, 1)

            return 0

        lax.fori_loop(0, QUAD, chunk, 0)

        @pl.when(f == 0)
        def _():
            weight_work(0)

        return 0

    def weight_work(f):
        def columns(m, _):
            cols = pl.ds(pl.multiple_of(m * (width // 2), width // 2), width // 2)
            both_v[f, cols] = tn(n_rows[:, cols], both_d[f % 2]).astype(low)
            down_v[f, :, cols] = tn(active[f % 2], g_rows[:, cols]).astype(low)
            return 0

        lax.fori_loop(0, 2, columns, 0)

        for copy in stage_copies(f):
            copy.start()

    def stage_copies(f):
        if f == 0:
            return []
        return [
            pltpu.make_async_copy(both_v.at[f], both_g.at[f - 1], stage_sem.at[0, f]),
            pltpu.make_async_copy(down_v.at[f], down_g.at[f - 1], stage_sem.at[1, f]),
        ]

    lax.fori_loop(0, tiles.count, tile_work, 0)

    half = members // 2
    lax.fori_loop(1, members, start_c, 0)
    c_in[plane] = c_sum[plane]
    weight_work(1)
    add_n(at.near(2))
    dn.start(0, 2)
    add_n(at.quad)
    dn.start(0, 0)
    weight_work(2)
    lax.fori_loop(0, half, give_y, 0)
    for step in range(len(dn.chip_bits)):
        dn.next(step)
    n_total[...] = dn.result()[0]
    for j in (half - 2, half - 1):
        y_copies(j)[0].wait()
    for f in range(tiles.count):
        for copy in stage_copies(f):
            copy.wait()

    def core_in(j, _):
        y_copies(j)[1].wait_send()
        arrived(y_far.at[j], far_sem.at[1, 1, j])
        return 0

    lax.fori_loop(0, half, core_in, 0)

    def c_done(k, _):
        c_copy(k).wait_send()
        other = (plane + k) % members
        arrived(c_in.at[other], c_sem.at[1, other])
        return 0

    lax.fori_loop(1, members, c_done, 0)
    dn.finish()
    home.arrive()
    incoming.sent()
    home.sent()


def expert_call(grps, exps, cap, deal, routes_t, comb_all, n_all, cot_all, both_w, down_w, in_low, down_slab, h1):
    members, rows, width = n_all.shape
    reps = grps * QUAD
    tiles = Tiles(down_slab.shape[0], reps)
    size = tiles.size
    slab, both_hidden = in_low.shape
    units = down_slab.shape[0]
    slots = exps * cap
    chip_bits = bits_of(members) - 1
    shape = jax.ShapeDtypeStruct
    vmem = pl.BlockSpec(memory_space=pltpu.VMEM)
    smem = pl.BlockSpec(memory_space=pltpu.SMEM)
    hbm = pl.BlockSpec(memory_space=pl.ANY)
    results = [
        (shape((rows, width), low), vmem),
        (shape((members // 2, rows, width), low), hbm),
        (shape((members // 2, rows, width), low), hbm),
        (shape((members, 8, rows), full), vmem),
        (shape((2, width, 2 * size), low), hbm),
        (shape((2, size, width), low), hbm),
        (shape((grps, slab, both_hidden), low), hbm),
        (shape((grps, units, width), low), hbm),
    ]
    dma = pltpu.SemaphoreType.DMA
    return pl.pallas_call(
        functools.partial(expert_kernel, grps, exps, cap),
        out_shape=[r[0] for r in results],
        in_specs=[smem] + [vmem] * 2 + [hbm] * 6 + [vmem],
        out_specs=[r[1] for r in results],
        scratch_shapes=[
            pltpu.VMEM((members, cap, rows), low),
            pltpu.VMEM((QUAD * slots, 128), full),
            pltpu.VMEM((QUAD * slots, width), low),
            pltpu.VMEM((QUAD * slots, width), low),
            pltpu.VMEM((tiles.count, width, 2 * size), low),
            pltpu.VMEM((tiles.count, size, width), low),
            pltpu.VMEM((2 * exps, rows, width), low),
            pltpu.VMEM((2 * exps, rows, width), low),
            pltpu.VMEM((QUAD * slots, width), low),
            pltpu.VMEM((QUAD * slots, width), low),
            pltpu.VMEM((2, QUAD * slots, 2 * size), low),
            pltpu.VMEM((2, QUAD * slots, size), low),
            [pltpu.VMEM((members >> (1 + step), rows, width), low) for step in range(chip_bits + 1)],
            pltpu.VMEM((members, 8, rows), full),
            pltpu.VMEM((2, rows, width), low),
            dma((2, 2)),
            dma((2, 2)),
            dma((2,)),
            dma((2, 2 * reps)),
            dma((2, reps + 1)),
            dma((2, 2 * reps)),
            dma((2, max(QUAD, grps))),
            dma((2, tiles.count)),
            dma((2, 2, members // 2)),
            dma((2, 3 << chip_bits)),
            dma((2, members)),
        ],
        compiler_params=pltpu.CompilerParams(
            collective_id=2, has_side_effects=True, vmem_limit_bytes=60 * 1024 * 1024
        ),
        name="experts",
    )(deal, routes_t, comb_all, n_all, cot_all, both_w, down_w, in_low, down_slab, h1)


def adamw_root(weight, moment, second, gradient, step_rate, decay_factor):
    new_moment = beta_one * moment + (1.0 - beta_one) * gradient
    new_second = beta_two * second + (1.0 - beta_two) * gradient * gradient
    root = lax.rsqrt(new_second * (1.0 / (1.0 - beta_two**STEP)))
    step = new_moment * (root * (1.0 - eps_adam * root))
    keep = 1.0 - step_rate * decay_factor
    return (new_moment, new_second, keep * weight - (step_rate / (1.0 - beta_one**STEP)) * step)


def adam_kernel(exps, *refs):
    in_parts, down_parts, qkv_grad, out_grad, small = refs[:5]
    states, news, bias_grad = refs[5:26], refs[26:47], refs[47]
    heads = HEADS // exps
    width = small.shape[1]

    def update(i, grad, rate, decay):
        weight, first, second = [state[...] for state in states[3 * i : 3 * i + 3]]
        values = adamw_root(weight, first, second, grad, rate, decay)
        for new, value in zip(news[3 * i : 3 * i + 3], values, strict=True):
            new[...] = value

    def total(parts):
        result = parts[0].astype(full)
        for k in range(1, parts.shape[0]):
            result = result + parts[k].astype(full)
        return result

    @pl.when(pl.program_id(0) == 0)
    def _():
        update(0, qkv_grad[...], 1.5 / math.sqrt(D), 0.1)
        update(1, out_grad[...], 6.0 / math.sqrt(D), 0.1)
        for e in range(exps):
            for h in range(heads):
                bias_grad[e * heads + h : e * heads + h + 1, :] = small[
                    exps + 3 + e : exps + 4 + e, h * 128 : h * 128 + BUCKETS
                ]
        update(2, bias_grad[...], 0.3, 0.0)
        update(3, small[0:exps, :], 1.0 / math.sqrt(D), 0.1)
        update(4, small[exps : exps + 2, :], 0.5, 0.0)

    update(5, total(in_parts), 1.5 / math.sqrt(D), 0.1)
    update(6, total(down_parts), 1.5 / math.sqrt(FF), 0.1)


def adam_call(exps, in_parts, down_parts, qkv_grad, out_grad, small, states):
    steps = 4

    def whole(array):
        return pl.BlockSpec(array.shape, lambda i: (0,) * array.ndim)

    def columns(array):
        block = array.shape[:-1] + (array.shape[-1] // steps,)
        return pl.BlockSpec(block, lambda i: (0,) * (array.ndim - 1) + (i,))

    specs = [whole(state) for state in states[:15]]
    specs += [columns(state) for state in states[15:18]] + [columns(state) for state in states[18:]]
    return pl.pallas_call(
        functools.partial(adam_kernel, exps),
        grid=(steps,),
        in_specs=[columns(in_parts), columns(down_parts), whole(qkv_grad), whole(out_grad), whole(small)] + specs,
        out_specs=specs,
        out_shape=[jax.ShapeDtypeStruct(state.shape, full) for state in states],
        scratch_shapes=[pltpu.VMEM((HEADS, BUCKETS), full)],
        compiler_params=pltpu.CompilerParams(vmem_limit_bytes=60 * 1024 * 1024),
        name="adam",
    )(in_parts, down_parts, qkv_grad, out_grad, small, *states)


def backward_kernel(
    grps,
    exps,
    lengths,
    deal,
    y_half,
    y_far,
    both_g,
    down_g,
    in_before,
    down_before,
    n1_in,
    cot_all,
    routes_t,
    tokens,
    n_total,
    c_in,
    n2_in,
    probs_in,
    h1_from,
    qkv_from,
    pb_from,
    mine_from,
    wqkv_from,
    wout_from,
    gains,
    router_t,
    *rest,
):
    token_grad, block_out, in_parts, down_parts, qkv_grad, out_grad, small_out = rest[:7]
    scratch = rest[7:]
    (
    h1_in,
    qkv,
    pb,
    mine,
    wqkv,
    wout,
    kept,
    y_bufs,
    dh1,
    dz_send,
    dz_all,
    do_send,
    do_in,
    bias_sum,
    dqkv,
    dqkv_t,
    dn1_send,
    dn1_in,
    wq_send,
    og_send,
    mids,
    far_send,
    far_in,
    small_send,
    small_exp,
    small_sum,
    small_rep,
    small_half,
    small_far,
    y_sem,
    load_sem,
    weight_sem,
    down_sem,
    dz_sem,
    do_sem,
    dn1_sem,
    wq_sem,
    og_sem,
    mid_sem,
    far_sem,
    small_sem,
    small2_sem,
    small3_sem,
    n1_sem,
    operand_sem,
    ) = scratch
    at = Where(grps, exps)
    reps = at.reps
    rows, width = tokens.shape
    heads = HEADS // exps
    head_dim = width // HEADS
    head_cols = heads * head_dim
    block_cols = min(128, head_cols)
    row_block = wqkv.shape[2]
    out_cols = wout.shape[3]
    tiles = Tiles(down_parts.shape[1], reps)
    scale = 1.0 / math.sqrt(head_dim)
    SEND, RECV = 0, 1
    plane = at.quad * exps + at.exp
    members = QUAD * exps

    def exp_peer(k):
        return (at.exp + k) % exps

    router = router_t[...]
    met = greet(*neighbours(at))
    n1 = kept.at[0:exps]
    group = pl.ds(pl.multiple_of(at.quad * exps, exps), exps)
    cot_copy = pltpu.make_async_copy(cot_all.at[group], dn1_send, n1_sem.at[1])
    cot_copy.start()
    loads = [
        pltpu.make_async_copy(src, dst, operand_sem.at[i])
        for i, (src, dst) in enumerate(
            ((h1_from, h1_in), (wout_from, wout), (qkv_from, qkv), (pb_from, pb), (mine_from, mine), (wqkv_from, wqkv))
        )
    ]
    ys = Halving(at, y_bufs, y_sem, [[0, 1, 2], [1, 2, 0], [2, 0, 1]])
    half_loads = [
        pltpu.make_async_copy(y_far, y_bufs[0], load_sem.at[0]),
        pltpu.make_async_copy(y_half, kept, load_sem.at[1]),
    ]
    for copy in loads + half_loads:
        copy.start()

    span = 2 * rows
    met()

    homes = [
        Homeward(
            at, tiles, t + 1, both_g.at[t], down_g.at[t], in_parts, down_parts, weight_sem.at[t], down_sem.at[t]
        )
        for t in range(2)
    ]
    homes[0].start()
    n1_copy = pltpu.make_async_copy(n1_in, n1, n1_sem.at[0])

    lane = lane_of((rows, 128))
    comb_rows = []
    for e in range(exps):
        total = c_in[e]
        for q in range(1, QUAD):
            total = total + c_in[q * exps + e]
        comb_rows.append(total[0:1, :])
    comb_rows.append(jnp.zeros((128 - exps, rows), full))
    comb_grad = jnp.concatenate(comb_rows, axis=0).T
    valid = row_of((rows, 1)) < lengths[at.me]
    probs = probs_in[...]
    hot = routed(routes_t, at.me, rows)
    picked = jnp.where(hot, probs, 0.0)
    total = jnp.sum(picked, axis=1, keepdims=True)
    gate = picked / total
    gate_grad_rows = jnp.where(valid, comb_grad, 0.0)
    spread_grad = jnp.sum(gate_grad_rows * gate, axis=1, keepdims=True)
    probs_grad = jnp.where(hot, (gate_grad_rows - spread_grad) / total, 0.0)
    logit_grad = probs * (probs_grad - jnp.sum(probs_grad * probs, axis=1, keepdims=True))
    small_rows = small_send.shape[0]
    small_send[...] = jnp.zeros_like(small_send)
    router_back = jnp.dot(
        logit_grad, jnp.concatenate([router, jnp.zeros((128 - exps, width), full)], axis=0),
        precision=highest, preferred_element_type=full,
    )
    for copy in loads:
        copy.wait()
    h1 = h1_in[...]
    r2 = lax.rsqrt(jnp.mean(h1 * h1, axis=1, keepdims=True) + eps_norm)

    steps = len(ys.chip_bits)
    n2_grad = router_back + n_total[...].astype(full)
    scaled = n2_grad * gains[1:2, :]
    cot_copy.wait()
    dealt = deal[at.me] - at.base
    g = dn1_send[0]
    for e in range(1, exps):
        g = jnp.where(dealt == e, dn1_send[e], g)
    hidden_grad = (
        jnp.where(valid, g.astype(full), 0.0)
        + r2 * scaled
        - h1 * (r2 * r2 * r2) * jnp.mean(scaled * h1, axis=1, keepdims=True)
    )
    dh1[...] = hidden_grad
    small_send[exps + 1 : exps + 2, :] = jnp.sum(n2_grad * h1 * r2, axis=0, keepdims=True)
    branch = hidden_grad.astype(low)
    dz_send[...] = branch
    for e in range(exps):
        total = jnp.zeros((rows, row_block), full)
        for r in range(reps):
            total = total + nt(branch[:, r * out_cols : (r + 1) * out_cols], wout[e, r])
        do_send[e] = total.astype(low)

    def do_copies():
        return [
            send(
                do_send.at[exp_peer(k)],
                do_in.at[at.exp],
                do_sem.at[SEND, exp_peer(k)],
                do_sem.at[RECV, at.exp],
                at.device(at.rep, exp_peer(k)),
            )
            for k in range(1, exps)
        ]

    for copy in do_copies():
        copy.start()
    pltpu.make_async_copy(do_send.at[at.exp], do_in.at[at.exp], do_sem.at[RECV, at.exp]).start()

    group_dz = Group(at, dz_send, dz_all, dz_sem)
    dz_all[at.exp] = branch
    for copy in half_loads:
        copy.wait()

    def add_halves(j, _):
        y_bufs[0][j] = y_bufs[0][j] + kept[j]
        return 0

    lax.fori_loop(0, kept.shape[0], add_halves, 0)
    n1_copy.start()

    bias_sum[...] = jnp.zeros_like(bias_sum)

    def dn1_copies():
        beside, across = turn(at.exp, 2), turn(at.exp, 1)
        return [
            functools.partial(
                send, dn1_send.at[k], dn1_in.at[j], dn1_sem.at[SEND, j], dn1_sem.at[RECV, j], at.device(at.rep, to)
            )
            for k, j, to in ((turn(at.exp, 0), 2, beside), (across, 0, across), (beside, 1, beside))
        ]

    def attend_back(i, _):
        s = turn(at.exp, i)
        arrived(do_in.at[s], do_sem.at[RECV, s])

        @pl.when(i == 0)
        def _():
            group_dz.start()
            ys.start(0)

        @pl.when(i == 2)
        def _():
            group_dz.pass_on()

        block_lane = lane_of((rows, block_cols))
        for c in range(head_cols // block_cols):
            cols = slice(c * block_cols, (c + 1) * block_cols)
            k_cols = slice(head_cols + c * block_cols, head_cols + (c + 1) * block_cols)
            v_cols = slice(2 * head_cols + c * block_cols, 2 * head_cols + (c + 1) * block_cols)
            q = qkv[s, :, cols] * scale
            k = qkv[s, :, k_cols]
            v = qkv[s, :, v_cols]
            do = do_in[s, :, cols]
            dq = jnp.zeros((rows, block_cols), full)
            dk = jnp.zeros((rows, block_cols), full)
            dv = jnp.zeros((rows, block_cols), full)
            for t in range(block_cols // head_dim):
                h = c * (block_cols // head_dim) + t
                here = jnp.logical_and(block_lane >= t * head_dim, block_lane < (t + 1) * head_dim)
                zero = jnp.zeros_like(q)
                do_h = jnp.where(here, do, zero)
                weights = pb[s * heads + h]
                p = weights.astype(full)
                dp = nt(do_h, v)
                delta = jnp.sum(dp * p, axis=1, keepdims=True)
                ds = (p * (dp - delta)).astype(low)
                bias_sum[h] += ds.astype(full)
                dv = jnp.where(here, tn(weights, do), dv)
                dq = jnp.where(here, jnp.dot(ds, k, preferred_element_type=full), dq)
                dk = jnp.where(here, tn(ds, q), dk)
            dqkv[:, cols] = (dq * scale).astype(low)
            dqkv[:, k_cols] = dk.astype(low)
            dqkv[:, v_cols] = dv.astype(low)
        dqkv_t[:, pl.ds(pl.multiple_of(s * rows, rows), rows)] = dqkv[...].T
        for e in range(exps):
            dn1_send[s, :, e * row_block : (e + 1) * row_block] = jnp.dot(
                dqkv[...], wqkv[e], preferred_element_type=full
            ).astype(low)

        @pl.when(i == 0)
        def _():
            dn1_copies()[0]().start()

        @pl.when(i == 1)
        def _():
            arrived(dn1_in.at[2], dn1_sem.at[RECV, 2])
            dn1_send[s] = (dn1_send[s].astype(full) + dn1_in[2].astype(full)).astype(low)
            dn1_copies()[1]().start()

        @pl.when(i == 2)
        def _():
            dn1_copies()[2]().start()

        return 0

    lax.fori_loop(0, exps, attend_back, 0)

    n1_copy.wait()
    seg = wq_send.shape[2]
    parts = wq_send.shape[1]
    segs = mids.shape[1] - 1
    for e in range(exps):
        part = kept[0:exps, :, e * row_block : (e + 1) * row_block].reshape(exps * rows, row_block)
        total = dot(dqkv_t[...], part)
        for j in range(parts):
            wq_send[e, j] = total[j * seg : (j + 1) * seg].astype(low)

    def owner(j):
        section, within = j // (head_cols // seg), j % (head_cols // seg)
        col = section * width + at.exp * head_cols + within * seg
        block = col // seg
        return block // segs, block % segs

    def mid_place(grp, k, quad):
        return (grp * (segs + 1) + k) * QUAD + quad

    def mid_copy(src, send_sem, rep, k, e):
        dst = mids.at[rep // QUAD, k, at.quad]
        recv = mid_sem.at[mid_place(rep // QUAD, k, at.quad)]
        stays = jnp.logical_and(rep % QUAD == at.quad, e == at.exp)
        return (
            stays,
            functools.partial(send, src, dst, send_sem, recv, (at.grp, rep % QUAD, e)),
            functools.partial(pltpu.make_async_copy, src, dst, recv),
        )

    def wq_copy(i):
        e, j = i // parts, i % parts
        rep, k = owner(j)
        return mid_copy(wq_send.at[e, j], wq_sem.at[i], rep, k, e)

    def og_copy(r):
        return mid_copy(og_send.at[r], og_sem.at[r], r, segs, at.exp)

    def go(copies, act, act_local):
        stays, away, local = copies

        @pl.when(jnp.logical_not(stays))
        def _():
            act(away)

        if act_local:

            @pl.when(stays)
            def _():
                act_local(local)

    def over(count, copies, act, act_local):
        def one(i, _):
            go(copies(i), act, act_local)
            return 0

        lax.fori_loop(0, count, one, 0)

    over(exps * parts, wq_copy, lambda copy: copy().start(), lambda copy: copy().start())
    group_dz.arrive()
    grad = tn(mine[...].reshape(exps * rows, head_cols), dz_all[...].reshape(exps * rows, width))
    for r in range(reps):
        og_send[r] = grad[:, r * out_cols : (r + 1) * out_cols].T.astype(low)
    over(reps, og_copy, lambda copy: copy().start(), lambda copy: copy().start())
    ys.next(0)
    homes[1].start()

    n1_grad = dn1_send[at.exp].astype(full)
    for j in range(2):
        arrived(dn1_in.at[j], dn1_sem.at[RECV, j])
        n1_grad = n1_grad + dn1_in[j].astype(full)
    x = tokens[...].astype(full)
    r1 = lax.rsqrt(jnp.mean(x * x, axis=1, keepdims=True) + eps_norm)
    scaled = n1_grad * gains[0:1, :]
    token_grad[...] = (
        dh1[...] + r1 * scaled - x * (r1 * r1 * r1) * jnp.mean(scaled * x, axis=1, keepdims=True)
    )
    small_send[exps : exps + 1, :] = jnp.sum(n1_grad * x * r1, axis=0, keepdims=True)

    ys.next(1)
    router_rows = lax.dot_general(
        logit_grad, n2_in[...].astype(full), (((0,), (0,)), ((), ())), preferred_element_type=full, precision=highest
    )
    small_send[0:exps, :] = router_rows[0:exps, :]

    flip = jnp.where(row_of((rows, rows)) + lane_of((rows, rows)) == rows - 1, 1.0, 0.0).astype(low)
    diagonals = []
    for h in range(heads):
        high = bias_sum[h].astype(low)
        rest = (bias_sum[h] - high.astype(full)).astype(low)
        flipped = dot(high, flip) + dot(rest, flip)
        square = jnp.concatenate([flipped, jnp.zeros((rows, rows), full)], axis=1)
        turned = pltpu.roll(square, 0, 1, stride=1, stride_axis=0)
        diagonals.append(jnp.sum(turned, axis=0, keepdims=True))
    diagonals = jnp.concatenate(diagonals + [jnp.zeros((8 - heads, span), full)], axis=0)
    in_bucket = jnp.where(bucket_of(rows - 1 - row_of((span, 128))) == lane_of((span, 128)), 1.0, 0.0)
    bias_line = jnp.dot(diagonals, in_bucket, precision=highest, preferred_element_type=full)
    for h in range(heads):
        small_send[exps + 2 : exps + 3, h * 128 : (h + 1) * 128] = bias_line[h : h + 1, :]

    def small_copies():
        return [
            send(
                small_send,
                small_exp.at[at.exp],
                small_sem.at[SEND, exp_peer(k)],
                small_sem.at[RECV, at.exp],
                at.device(at.rep, exp_peer(k)),
            )
            for k in range(1, exps)
        ]

    for copy in small_copies():
        copy.start()
    small_exp[at.exp] = small_send[...]

    def mid_sum(grp, k):
        for q in range(QUAD):
            arrived(mids.at[grp, k, q], mid_sem.at[mid_place(grp, k, q)])
        total = mids[grp, k, 0].astype(full)
        for q in range(1, QUAD):
            total = total + mids[grp, k, q].astype(full)
        return total

    far = 1 - at.grp
    for k in range(segs + 1):
        far_send[k] = mid_sum(far, k).astype(low)

    def far_copy():
        return send(far_send, far_in, far_sem.at[SEND], far_sem.at[RECV], (far, at.quad, at.exp))

    far_copy().start()
    for k in range(1, exps):
        arrived(small_exp.at[exp_peer(k)], small_sem.at[RECV, exp_peer(k)])
    total = small_exp[0]
    for e in range(1, exps):
        total = total + small_exp[e]
    small_sum[...] = total
    for e in range(exps):
        small_sum[exps + 3 + e : exps + 4 + e, :] = small_exp[e, exps + 2 : exps + 3, :]

    def small2_copies():
        return [
            send(
                small_sum,
                small_rep.at[at.quad],
                small2_sem.at[SEND, k - 1],
                small2_sem.at[RECV, at.quad],
                (at.grp, (at.quad + k) % QUAD, at.exp),
            )
            for k in range(1, QUAD)
        ]

    def small3_copy():
        return send(small_half, small_far, small3_sem.at[SEND], small3_sem.at[RECV], (far, at.quad, at.exp))

    for copy in small2_copies():
        copy.start()
    small_rep[at.quad] = small_sum[...]
    for step in range(2, steps):
        ys.next(step)
    length = lengths[at.base]
    for e in range(1, exps):
        length = jnp.where(deal[at.base + e] == at.me, lengths[at.base + e], length)
    block = ys.result()[0]
    block_out[...] = jnp.where(row_of((rows, 1)) < length, block, jnp.zeros_like(block))
    for k in range(1, QUAD):
        arrived(small_rep.at[(at.quad + k) % QUAD], small2_sem.at[RECV, (at.quad + k) % QUAD])
    total = small_rep[0]
    for q in range(1, QUAD):
        total = total + small_rep[q]
    small_half[...] = total
    small3_copy().start()
    arrived(small_far, small3_sem.at[RECV])
    total = small_half[...] + small_far[...]
    small_out[...] = total

    near = [mid_sum(at.grp, k) for k in range(segs + 1)]
    arrived(far_in, far_sem.at[RECV])
    grads = [(near[k] + far_in[k].astype(full)).T for k in range(segs + 1)]
    qkv_grad[...] = jnp.concatenate(grads[:segs], axis=1)
    out_grad[...] = grads[segs]
    for home in homes:
        home.arrive()

    ys.finish()

    for home in homes:
        home.sent()

    over(exps * parts, wq_copy, lambda copy: copy().wait_send(), None)
    over(reps, og_copy, lambda copy: copy().wait_send(), None)
    far_copy().wait_send()
    small3_copy().wait_send()
    for copies in (do_copies(), small_copies(), small2_copies()):
        for copy in copies:
            copy.wait_send()
    for copy in dn1_copies():
        copy().wait_send()
    group_dz.sent()


def routed(routes_t, seq, rows):
    pair = routes_t[:, pl.ds(pl.multiple_of(seq * rows, rows), rows)].astype(full)
    cols = jnp.concatenate([pair, jnp.zeros((126, rows), full)], axis=0).T
    lane = lane_of((rows, 128)).astype(full)
    return jnp.logical_or(lane == cols[:, 0:1], lane == cols[:, 1:2])


def backward_call(
    grps, exps, lengths, deal, y_half, y_far, both_g, down_g, in_before, down_before, n1,
    cot_all, routes_t, tokens, n_total, c_in, n2, probs, h1, qkv, pb, mine, wqkv, wout, gains, router
):
    reps = grps * QUAD
    rows, width = tokens.shape
    heads = HEADS // exps
    head_cols = width // exps
    row_block = wqkv.shape[2]
    out_cols = wout.shape[3]
    shard_cols = 3 * width // reps
    seg = math.gcd(shard_cols, head_cols)
    segs = shard_cols // seg
    parts = 3 * head_cols // seg
    members = QUAD * exps
    chip_bits = bits_of(members) - 1
    small_rows = -(-(2 * exps + 3) // 8) * 8
    shape = jax.ShapeDtypeStruct
    vmem = pl.BlockSpec(memory_space=pltpu.VMEM)
    smem = pl.BlockSpec(memory_space=pltpu.SMEM)
    hbm = pl.BlockSpec(memory_space=pl.ANY)
    results = [
        (shape((rows, width), full), vmem),
        (shape((rows, width), low), vmem),
        (shape(in_before.shape, low), hbm),
        (shape(down_before.shape, low), hbm),
        (shape((row_block, shard_cols), full), vmem),
        (shape((row_block, out_cols), full), vmem),
        (shape((small_rows, width), full), vmem),
    ]
    dma = pltpu.SemaphoreType.DMA
    bufs = [pltpu.VMEM((1 << (chip_bits - s), rows, width), low) for s in range(chip_bits + 1)]
    return pl.pallas_call(
        functools.partial(backward_kernel, grps, exps),
        out_shape=[r[0] for r in results],
        in_specs=[smem] * 2 + [hbm] * 8 + [vmem] * 6 + [hbm] * 6 + [vmem] * 2,
        out_specs=[r[1] for r in results],
        scratch_shapes=[
            pltpu.VMEM(h1.shape, full),
            pltpu.VMEM(qkv.shape, low),
            pltpu.VMEM(pb.shape, low),
            pltpu.VMEM(mine.shape, low),
            pltpu.VMEM(wqkv.shape, low),
            pltpu.VMEM(wout.shape, low),
            pltpu.VMEM((members // 2, rows, width), low),
            list(bufs),
            pltpu.VMEM((rows, width), full),
            pltpu.VMEM((rows, width), low),
            pltpu.VMEM((exps, rows, width), low),
            pltpu.VMEM((exps, rows, head_cols), low),
            pltpu.VMEM((exps, rows, head_cols), low),
            pltpu.VMEM((heads, rows, rows), full),
            pltpu.VMEM((rows, 3 * head_cols), low),
            pltpu.VMEM((3 * head_cols, exps * rows), low),
            pltpu.VMEM((exps, rows, width), low),
            pltpu.VMEM((3, rows, width), low),
            pltpu.VMEM((exps, parts, seg, row_block), low),
            pltpu.VMEM((reps, seg, row_block), low),
            pltpu.VMEM((grps, segs + 1, QUAD, seg, row_block), low),
            pltpu.VMEM((segs + 1, seg, row_block), low),
            pltpu.VMEM((segs + 1, seg, row_block), low),
            pltpu.VMEM((small_rows, width), full),
            pltpu.VMEM((exps, small_rows, width), full),
            pltpu.VMEM((small_rows, width), full),
            pltpu.VMEM((QUAD, small_rows, width), full),
            pltpu.VMEM((small_rows, width), full),
            pltpu.VMEM((small_rows, width), full),
            dma((2, 3 << chip_bits)),
            dma((2,)),
            dma((2, 2, 2 * reps)),
            dma((2, 2, max(QUAD, grps))),
            dma((2, exps)),
            dma((2, exps)),
            dma((2, exps)),
            dma((exps * parts,)),
            dma((reps,)),
            dma((grps * (segs + 1) * QUAD,)),
            dma((2,)),
            dma((2, exps)),
            dma((2, QUAD)),
            dma((2,)),
            dma((2,)),
            dma((6,)),
        ],
        compiler_params=pltpu.CompilerParams(
            collective_id=1, has_side_effects=True, vmem_limit_bytes=60 * 1024 * 1024
        ),
        input_output_aliases={6: 2, 7: 3},
        name="backward",
    )(
        lengths, deal, y_half, y_far, both_g, down_g, in_before, down_before, n1, cot_all,
        routes_t, tokens, n_total, c_in, n2, probs, h1, qkv, pb, mine, wqkv, wout, gains, router
    )


def per_device(
    tokens,
    cotangent,
    seq_lengths,
    deal,
    routes,
    attn_qkv,
    qkv_first,
    qkv_second,
    attn_out,
    out_first,
    out_second,
    rel_bias,
    bias_first,
    bias_second,
    router,
    router_first,
    router_second,
    norm_gains,
    gains_first,
    gains_second,
    expert_in,
    in_first,
    in_second,
    expert_out,
    down_first,
    down_second,
):
    rows, width = tokens.shape
    experts = router.shape[1]
    capacity = (10 * rows + 4 * experts - 1) // (4 * experts)
    exps = lax.axis_size("exp")
    grps = lax.axis_size("grp")
    routes_t = routes.T
    bias_table = rel_bias.T
    (
        both_w, down_w, cot_all, n_all, comb_all, qkv, pb, context_mine, normed_group, wqkv, wout, hidden_one,
        normed_two, router_probs, in_low, down_low,
    ) = forward_call(
        grps, exps, seq_lengths, bias_table, routes_t, tokens, cotangent, norm_gains.T, router.T,
        attn_qkv, attn_out, expert_in[0], expert_out[0],
    )
    n_total, y_half, y_far, c_in, both_g, down_g, in_before, down_before = expert_call(
        grps, exps, capacity, deal, routes_t, comb_all, n_all, cot_all, both_w, down_w, in_low, down_low,
        hidden_one,
    )
    token_grad, block_out, in_parts, down_parts, qkv_grad, out_grad, small = backward_call(
        grps, exps, seq_lengths, deal, y_half, y_far, both_g, down_g,
        in_before, down_before, normed_group, cot_all, routes_t, tokens, n_total, c_in, normed_two, router_probs, hidden_one, qkv, pb, context_mine, wqkv,
        wout, norm_gains.T, router.T,
    )
    states = [
        attn_qkv, qkv_first, qkv_second, attn_out, out_first, out_second, bias_table, bias_first.T, bias_second.T,
        router.T, router_first.T, router_second.T, norm_gains.T, gains_first.T, gains_second.T,
        expert_in[0], in_first[0], in_second[0], expert_out[0], down_first[0], down_second[0],
    ]
    new = list(adam_call(exps, in_parts, down_parts, qkv_grad, out_grad, small, states))
    new = new[:6] + [array.T for array in new[6:15]] + [array[None] for array in new[15:]]
    return (block_out, token_grad, *new)


def bucket_onehot(length):
    places = jnp.arange(length, dtype=jnp.int32)
    offset = places[None, :] - places[:, None]
    distance = jnp.abs(offset)
    bucket = 16 * (offset > 0).astype(jnp.int32)
    for threshold in thresholds:
        bucket = bucket + (distance >= threshold).astype(jnp.int32)
    return (bucket[:, :, None] == jnp.arange(BUCKETS, dtype=jnp.int32)[None, None, :]).astype(full)


def swap(pieces, axes):
    return lax.all_to_all(pieces, axes, split_axis=0, concat_axis=0, tiled=True)


def spread(block, axes):
    members = lax.axis_size(axes)
    return swap(jnp.broadcast_to(block[None], (members,) + block.shape), axes)


def plain_device(
    tokens,
    cotangent,
    seq_lengths,
    deal,
    routes,
    attn_qkv,
    qkv_first,
    qkv_second,
    attn_out,
    out_first,
    out_second,
    rel_bias,
    bias_first,
    bias_second,
    router,
    router_first,
    router_second,
    norm_gains,
    gains_first,
    gains_second,
    expert_in,
    in_first,
    in_second,
    expert_out,
    down_first,
    down_second,
):
    rows, width = tokens.shape
    head_dim = width // HEADS
    score_scale = 1.0 / math.sqrt(head_dim)
    experts = router.shape[1]
    capacity = (10 * rows + 4 * experts - 1) // (4 * experts)
    exps = lax.axis_size("exp")
    grps = lax.axis_size("grp")
    reps = grps * QUAD
    heads = HEADS // exps
    head_cols = heads * head_dim
    place = lax.axis_index("exp")
    base = lax.axis_index(REP) * exps
    me = base + place
    slab = expert_in.shape[1]
    units = expert_out.shape[1]
    quarter = grps * units

    row_block = attn_qkv.shape[0]
    qkv_rows = lax.all_gather(attn_qkv.astype(low), REP, axis=1, tiled=True)
    out_rows = lax.all_gather(attn_out.astype(low), REP, axis=1, tiled=True)
    qkv_pieces = jnp.transpose(
        qkv_rows.reshape(row_block, 3, exps, head_cols), (2, 0, 1, 3)
    ).reshape(exps, row_block, 3 * head_cols)
    qkv_mine = swap(qkv_pieces, "exp").reshape(width, 3 * head_cols)
    full_out = spread(out_rows, "exp").reshape(width, width)

    group_tokens = spread(tokens, "exp")
    group_cotangent = spread(cotangent, "exp")
    my_cotangent = lax.dynamic_index_in_dim(group_cotangent, deal[me] - base, 0, keepdims=False)

    my_routes = lax.dynamic_slice_in_dim(routes, me * rows, rows, 0)
    places = jnp.arange(rows, dtype=jnp.int32)
    valid_rows = (places < seq_lengths[me]).astype(full)
    group_lengths = lax.dynamic_slice_in_dim(seq_lengths, base, exps, 0)
    key_ok = places[None, :] < group_lengths[:, None]
    gain_one = norm_gains[:, 0]
    gain_two = norm_gains[:, 1]

    chosen = (my_routes[:, :, None] == jnp.arange(experts, dtype=jnp.int32)[None, None, :]).astype(full)
    flat_routes = my_routes.reshape(-1)
    route_hot = (flat_routes[:, None] == jnp.arange(experts, dtype=jnp.int32)[None, :]).astype(jnp.int32)
    before = jnp.cumsum(route_hot, axis=0) - route_hot
    slot_index = jnp.sum(before * route_hot, axis=-1)
    target = (flat_routes * capacity + slot_index).reshape(rows, 2)
    slots = experts * capacity
    slot_ids = jnp.arange(slots, dtype=jnp.int32)
    place_first = slot_ids[:, None] == target[None, :, 0]
    place_second = slot_ids[:, None] == target[None, :, 1]
    place_any = jnp.logical_or(place_first, place_second).astype(low)

    shard_in = expert_in[0].astype(low).reshape(slab, 2, grps, QUAD, units)
    in_pieces = jnp.transpose(shard_in, (1, 3, 0, 2, 4)).reshape(2, 1, QUAD, slab, quarter)
    in_pieces = jnp.broadcast_to(in_pieces, (2, grps, QUAD, slab, quarter)).reshape(
        2, reps, slab, quarter
    )
    down_mine = spread(expert_out[0].astype(low), "grp").reshape(quarter, width)
    gate_mine = swap(in_pieces[0], REP).reshape(width, quarter)
    up_mine = swap(in_pieces[1], REP).reshape(width, quarter)

    upstream = my_cotangent.astype(full) * valid_rows[:, None]

    def to_experts(block):
        sent = block.reshape((1, experts) + block.shape[1:])
        sent = jnp.broadcast_to(sent, (QUAD,) + sent.shape[1:])
        return swap(sent.reshape((QUAD * experts,) + block.shape[1:]), PLANE)

    def dispatch(values):
        return dot(place_any, values).astype(low).reshape(experts, capacity, width)

    expert_upstream = to_experts(dispatch(upstream.astype(low))).reshape(-1, width)
    active_grad_bare = lax.dot_general(
        expert_upstream, down_mine, (((1,), (1,)), ((), ())), preferred_element_type=full
    )

    x_group = group_tokens.astype(full)
    scale_group = lax.rsqrt(jnp.mean(x_group * x_group, axis=-1, keepdims=True) + eps_norm)
    normed_group = (x_group * scale_group * gain_one).astype(low).reshape(exps * rows, width)
    qkv = dot(normed_group, qkv_mine).astype(low).reshape(exps, rows, 3, heads, head_dim)
    queries = qkv[:, :, 0]
    key_rows = qkv[:, :, 1]
    values = qkv[:, :, 2]
    onehot = bucket_onehot(rows)
    bias_mine = lax.dynamic_slice_in_dim(rel_bias, place * heads, heads, 1)
    bias_table = jnp.einsum("ijb,bh->hij", onehot, bias_mine, precision=highest)

    def scores_of():
        raw = (
            jnp.einsum("sihd,sjhd->shij", queries, key_rows, preferred_element_type=full)
            * score_scale
            + bias_table[None]
        )
        return jnp.where(key_ok[:, None, None, :], raw, -1e30)

    scores = scores_of()
    row_max = jnp.max(scores, axis=-1, keepdims=True)
    log_total = row_max + jnp.log(jnp.sum(jnp.exp(scores - row_max), axis=-1, keepdims=True))
    weights_low = jnp.exp(scores - log_total).astype(low)
    context_mine = (
        jnp.einsum("shij,sjhd->sihd", weights_low, values, preferred_element_type=full)
        .astype(low)
        .reshape(exps, rows, head_cols)
    )
    context = jnp.transpose(swap(context_mine, "exp"), (1, 0, 2)).reshape(rows, width)

    x_float = tokens.astype(full)
    scale_one = lax.rsqrt(jnp.mean(x_float * x_float, axis=-1, keepdims=True) + eps_norm)
    hidden_one = x_float + dot(context, full_out)
    scale_two = lax.rsqrt(jnp.mean(hidden_one * hidden_one, axis=-1, keepdims=True) + eps_norm)
    normed_two = (hidden_one * scale_two * gain_two).astype(low)
    normed_float = normed_two.astype(full)
    router_probs = jax.nn.softmax(jnp.dot(normed_float, router, precision=highest), axis=-1)
    picked = jnp.sum(router_probs[:, None, :] * chosen, axis=-1)
    gate_total = jnp.sum(picked, axis=-1, keepdims=True)
    gate_value = picked / gate_total
    combine = gate_value * valid_rows[:, None]
    combine_slots = jnp.sum(
        jnp.where(place_first, combine[None, :, 0], 0.0)
        + jnp.where(place_second, combine[None, :, 1], 0.0),
        axis=1,
    ).reshape(experts, 1, capacity)

    expert_rows = to_experts(dispatch(normed_two)).reshape(-1, width)
    expert_combine = to_experts(combine_slots).reshape(-1, 1)

    gate_part = dot(expert_rows, gate_mine)
    up_part = dot(expert_rows, up_mine)
    active_float, active_pull = jax.vjp(gated_unit, gate_part, up_part)
    active = active_float.astype(low)
    active_scaled = (active_float * expert_combine).astype(low)
    combine_grad_part = jnp.sum(active_float * active_grad_bare, axis=-1).reshape(
        QUAD * experts, 1, capacity
    )
    gate_part_grad, up_part_grad = active_pull(active_grad_bare * expert_combine)
    gate_part_grad = gate_part_grad.astype(low)
    up_part_grad = up_part_grad.astype(low)
    rows_grad_part = (
        lax.dot_general(gate_part_grad, gate_mine, (((1,), (1,)), ((), ())), preferred_element_type=full)
        + lax.dot_general(up_part_grad, up_mine, (((1,), (1,)), ((), ())), preferred_element_type=full)
    ).astype(low)
    output_part = dot(active, down_mine).astype(low)

    combine_grad_back = swap(combine_grad_part, PLANE)
    rows_grad_back = swap(rows_grad_part.reshape(QUAD * experts, capacity, width), PLANE)
    output_back = swap(output_part.reshape(QUAD * experts, capacity, width), PLANE)

    def transposed_dot(a, b):
        return lax.dot_general(a, b, (((0,), (0,)), ((), ())), preferred_element_type=full)

    down_grad = transposed_dot(active_scaled, expert_upstream).astype(low)
    gate_grad = transposed_dot(expert_rows, gate_part_grad).astype(low)
    up_grad = transposed_dot(expert_rows, up_part_grad).astype(low)
    down_share = jnp.sum(
        swap(down_grad.reshape(grps, units, width), "grp").astype(full), axis=0
    )[None]

    def in_columns(grad):
        back = swap(grad.reshape(reps, slab, quarter), REP).astype(full)
        back = jnp.sum(back.reshape(grps, QUAD, slab, grps, units), axis=0)
        return jnp.transpose(back, (1, 2, 0, 3)).reshape(slab, grps * QUAD * units)

    in_share = jnp.concatenate([in_columns(gate_grad), in_columns(up_grad)], axis=1)[None]

    def from_slots(placed, parts):
        hot = jnp.broadcast_to(placed.astype(low)[None], (QUAD,) + placed.shape).reshape(-1, rows)
        return lax.dot_general(
            hot, parts.reshape(-1, width), (((0,), (0,)), ((), ())), preferred_element_type=full
        )

    mixture = combine[:, :1] * from_slots(place_first, output_back) + combine[:, 1:] * from_slots(
        place_second, output_back
    )
    block_loader = (valid_rows[:, None] * (hidden_one + mixture)).astype(low)
    seq_ids = jnp.arange(deal.shape[0], dtype=jnp.int32)
    dealt_seq = jnp.sum(jnp.where(deal == me, seq_ids, 0))
    block_out = lax.dynamic_index_in_dim(
        spread(block_loader, "exp"), dealt_seq - base, 0, keepdims=False
    )

    combine_grad_slots = jnp.sum(combine_grad_back.reshape(QUAD, slots), axis=0)
    combine_grad = jnp.stack(
        [
            jnp.sum(jnp.where(place_first, combine_grad_slots[:, None], 0.0), axis=0),
            jnp.sum(jnp.where(place_second, combine_grad_slots[:, None], 0.0), axis=0),
        ],
        axis=1,
    )
    gate_grad_value = combine_grad * valid_rows[:, None]
    picked_grad = (
        gate_grad_value - jnp.sum(gate_grad_value * gate_value, axis=-1, keepdims=True)
    ) / gate_total
    probs_grad = jnp.sum(picked_grad[:, :, None] * chosen, axis=1)
    logit_grad = router_probs * (
        probs_grad - jnp.sum(probs_grad * router_probs, axis=-1, keepdims=True)
    )
    router_grad = jnp.dot(normed_float.T, logit_grad, precision=highest)
    normed_grad = jnp.dot(logit_grad, router.T, precision=highest) + from_slots(
        jnp.logical_or(place_first, place_second), rows_grad_back
    )
    scaled_two = normed_grad * gain_two
    hidden_grad = (
        upstream
        + scale_two * scaled_two
        - hidden_one * scale_two**3 * jnp.mean(scaled_two * hidden_one, axis=-1, keepdims=True)
    )
    gain_two_grad = jnp.sum(normed_grad * hidden_one * scale_two, axis=0)
    branch_grad = hidden_grad.astype(low)
    context_grad = lax.dot_general(
        branch_grad, full_out, (((1,), (1,)), ((), ())), preferred_element_type=full
    ).astype(low)
    context_grad_pieces = jnp.transpose(context_grad.reshape(rows, exps, head_cols), (1, 0, 2))
    context_grad_mine = swap(context_grad_pieces, "exp").reshape(exps, rows, heads, head_dim)
    branch_group = spread(branch_grad, "exp").reshape(exps * rows, width)
    out_grad = transposed_dot(context_mine.reshape(exps * rows, head_cols), branch_group).astype(low)

    scores = scores_of()
    probs_again = jnp.exp(scores - log_total)
    weights_again = probs_again.astype(low)
    values_grad = jnp.einsum(
        "shij,sihd->sjhd", weights_again, context_grad_mine, preferred_element_type=full
    )
    probs_grad_att = jnp.einsum(
        "sihd,sjhd->shij", context_grad_mine, values, preferred_element_type=full
    )
    row_delta = jnp.sum(probs_grad_att * probs_again, axis=-1, keepdims=True)
    scores_grad = (probs_again * (probs_grad_att - row_delta)).astype(low)
    scores_grad_sum = jnp.sum(scores_grad.astype(full), axis=0)
    bias_grad_mine = jnp.einsum("hij,ijb->bh", scores_grad_sum, onehot, precision=highest)
    bias_grad = lax.dynamic_update_slice_in_dim(
        jnp.zeros((BUCKETS, HEADS), full), bias_grad_mine, place * heads, 1
    )
    queries_grad = (
        jnp.einsum("shij,sjhd->sihd", scores_grad, key_rows, preferred_element_type=full)
        * score_scale
    )
    keys_grad = (
        jnp.einsum("shij,sihd->sjhd", scores_grad, queries, preferred_element_type=full)
        * score_scale
    )
    qkv_grad = (
        jnp.stack([queries_grad, keys_grad, values_grad], axis=2)
        .astype(low)
        .reshape(exps * rows, 3 * head_cols)
    )
    normed_one_part = lax.dot_general(
        qkv_grad, qkv_mine, (((1,), (1,)), ((), ())), preferred_element_type=full
    ).astype(low)
    normed_one_grad = jnp.sum(
        swap(normed_one_part.reshape(exps, rows, width), "exp").astype(full), axis=0
    )
    scaled_one = normed_one_grad * gain_one
    token_grad = (
        hidden_grad
        + scale_one * scaled_one
        - x_float * scale_one**3 * jnp.mean(scaled_one * x_float, axis=-1, keepdims=True)
    )
    gain_one_grad = jnp.sum(normed_one_grad * x_float * scale_one, axis=0)

    qkv_weight_grad = transposed_dot(normed_group, qkv_grad).astype(low)
    qkv_grad_rows = swap(qkv_weight_grad.reshape(exps, row_block, 3 * head_cols), "exp")
    qkv_grad_rows = jnp.transpose(
        qkv_grad_rows.reshape(exps, row_block, 3, head_cols), (1, 2, 0, 3)
    ).reshape(row_block, reps, -1)
    qkv_share = jnp.sum(
        swap(jnp.transpose(qkv_grad_rows, (1, 0, 2)), REP).astype(full), axis=0
    )
    out_pieces = jnp.transpose(out_grad.reshape(row_block, reps, -1), (1, 0, 2))
    out_share = jnp.sum(swap(out_pieces, REP).astype(full), axis=0)

    small = jnp.concatenate(
        [
            router_grad.reshape(-1),
            jnp.stack([gain_one_grad, gain_two_grad], axis=1).reshape(-1),
            bias_grad.reshape(-1),
        ]
    ).reshape(-1, 128)
    small_total = jnp.sum(lax.all_gather(small, ALL, axis=0, tiled=False), axis=0).reshape(-1)
    router_total = small_total[: router.size].reshape(router.shape)
    gains_total = small_total[router.size : router.size + norm_gains.size].reshape(norm_gains.shape)
    bias_total = small_total[router.size + norm_gains.size :].reshape(rel_bias.shape)

    qkv_new = adamw_update(attn_qkv, qkv_first, qkv_second, qkv_share, 1.5 / math.sqrt(D), 0.1)
    out_new = adamw_update(attn_out, out_first, out_second, out_share, 6.0 / math.sqrt(D), 0.1)
    bias_new = adamw_update(rel_bias, bias_first, bias_second, bias_total, 0.3, 0.0)
    router_new = adamw_update(
        router, router_first, router_second, router_total, 1.0 / math.sqrt(D), 0.1
    )
    gains_new = adamw_update(norm_gains, gains_first, gains_second, gains_total, 0.5, 0.0)
    in_new = adamw_update(expert_in, in_first, in_second, in_share, 1.5 / math.sqrt(D), 0.1)
    down_new = adamw_update(
        expert_out, down_first, down_second, down_share, 1.5 / math.sqrt(FF), 0.1
    )
    return (
        (block_out, token_grad)
        + qkv_new
        + out_new
        + bias_new
        + router_new
        + gains_new
        + in_new
        + down_new
    )


def solution(mesh):
    reps, exps = mesh.devices.shape
    split = Mesh(mesh.devices.reshape(reps // QUAD, QUAD, exps), ALL)
    by_rows = P(ALL, None)
    attn = P("exp", REP)
    expert = P("exp", REP, None)
    return jax.shard_map(
        per_device if (reps, exps) == (2 * QUAD, 4) else plain_device,
        mesh=split,
        in_specs=(by_rows, by_rows) + (P(),) * 3 + (attn,) * 6 + (P(),) * 9 + (expert,) * 6,
        out_specs=(by_rows, by_rows) + (attn,) * 6 + (P(),) * 9 + (expert,) * 6,
        check_vma=False,
    )
```

```python
import functools
import math

import jax
import jax.numpy as jnp
from jax import lax
from jax.experimental import pallas as pl
from jax.experimental.pallas import tpu as pltpu
from jax.sharding import Mesh
from jax.sharding import PartitionSpec as P

D = 1024
HEADS = 16
FF = 2816
BUCKETS = 32
STEP = 10
QUAD = 4
REP = ("grp", "quad")
PLANE = ("quad", "exp")
ALL = ("grp", "quad", "exp")

highest = lax.Precision.HIGHEST
eps_norm = 1e-06
thresholds = (1, 2, 3, 4, 5, 6, 7, 8, 11, 16, 22, 32, 45, 64, 90)
beta_one = 0.9
beta_two = 0.999
eps_adam = 1e-08
low = jnp.bfloat16
full = jnp.float32
MESH = pl.DeviceIdType.MESH


def adamw_update(weight, moment, second, gradient, step_rate, decay_factor):
    new_moment = beta_one * moment + (1.0 - beta_one) * gradient
    new_second = beta_two * second + (1.0 - beta_two) * gradient * gradient
    corrected = new_moment / (1.0 - beta_one**STEP)
    scaled = new_second / (1.0 - beta_two**STEP)
    new_weight = weight - step_rate * (
        corrected / (jnp.sqrt(scaled) + eps_adam) + decay_factor * weight
    )
    return (new_moment, new_second, new_weight)


def gated_unit(gate_input, up_input):
    return jax.nn.gelu(gate_input, approximate=True) * up_input


def dot(a, b):
    return jnp.dot(a, b, preferred_element_type=full)


def nt(a, b, precision=None):
    return lax.dot_general(a, b, (((1,), (1,)), ((), ())), preferred_element_type=full, precision=precision)


def tn(a, b):
    return lax.dot_general(a, b, (((0,), (0,)), ((), ())), preferred_element_type=full)


class Where:
    def __init__(self, grps, exps):
        self.grps, self.exps = grps, exps
        self.reps = grps * QUAD
        self.grp = lax.axis_index("grp")
        self.quad = lax.axis_index("quad")
        self.exp = lax.axis_index("exp")
        self.rep = self.grp * QUAD + self.quad
        self.base = self.rep * exps
        self.me = self.base + self.exp

    def device(self, rep, exp):
        return (rep // QUAD, rep % QUAD, exp)

    def near(self, flip):
        q = self.quad
        if flip & 1:
            q = q + 1 - 2 * (q % 2)
        if flip & 2:
            q = q + 2 - 4 * (q // 2)
        return q


def send(src, dst, send_sem, recv_sem, device):
    return pltpu.make_async_remote_copy(
        src_ref=src, dst_ref=dst, send_sem=send_sem, recv_sem=recv_sem, device_id=device, device_id_type=MESH
    )


def arrived(ref, sem):
    pltpu.make_async_copy(ref, ref, sem).wait()


def greet(count, device):
    barrier = pltpu.get_barrier_semaphore()

    def one(k, _):
        pl.semaphore_signal(barrier, inc=1, device_id=device(k), device_id_type=MESH)
        return 0

    lax.fori_loop(1, count + 1, one, 0)
    return functools.partial(pl.semaphore_wait, barrier, count)


def everyone(at):
    count = at.reps * at.exps

    def device(k):
        other = (at.me + k) % count
        return at.device(other // at.exps, other % at.exps)

    return count - 1, device


def neighbours(at):
    members = QUAD * at.exps
    plane = at.quad * at.exps + at.exp

    def device(k):
        other = (plane + k) % members
        rest = k - members
        grp = jnp.where(k < members, at.grp, (at.grp + 1 + rest // QUAD) % at.grps)
        quad = jnp.where(k < members, other // at.exps, rest % QUAD)
        return grp, quad, jnp.where(k < members, other % at.exps, at.exp)

    return members - 1 + QUAD * (at.grps - 1), device


def turn(exp, i):
    beside = exp + 1 - 2 * (exp % 2)
    return jnp.where(i == 0, (beside + 2) % 4, jnp.where(i == 1, (exp + 2) % 4, jnp.where(i == 2, beside, exp)))


def lane_of(shape):
    return lax.broadcasted_iota(jnp.int32, shape, 1)


def row_of(shape):
    return lax.broadcasted_iota(jnp.int32, shape, 0)


def bucket_of(offset):
    distance = jnp.abs(offset)
    bucket = jnp.where(offset > 0, 16, 0)
    for threshold in thresholds:
        bucket = bucket + jnp.where(distance >= threshold, 1, 0)
    return bucket


def bits_of(count):
    return count.bit_length() - 1


def column_parts(width):
    tiles = width // 128
    cuts = [0, (tiles + 2) // 3, (2 * tiles + 2) // 3, tiles]
    return [(cuts[i] * 128, (cuts[i + 1] - cuts[i]) * 128) for i in range(3)]


def flipped(place, bit):
    return place + (1 - 2 * ((place // (1 << bit)) % 2)) * (1 << bit)


class Doubling:
    def __init__(self, at, own, every, sems, core_sems, orders):
        self.at, self.own, self.every = at, own, every
        self.sems, self.core_sems, self.orders = sems, core_sems, orders
        self.plane = at.quad * at.exps + at.exp
        self.steps = len(orders[0])
        self.parts = column_parts(own.shape[1])

    def device(self, bit):
        other = flipped(self.plane, bit)
        return (self.at.grp, other // self.at.exps, other % self.at.exps)

    def place(self, part, j):
        p = self.plane
        for i, bit in enumerate(self.orders[part]):
            if (j >> i) & 1:
                p = flipped(p, bit + 1)
        return p

    def block(self, part, p):
        begin, size = self.parts[part]
        return self.every.at[p, :, pl.ds(begin, size)]

    def source(self, part, j):
        begin, size = self.parts[part]
        return self.own.at[:, pl.ds(begin, size)] if j == 0 else self.block(part, self.place(part, j))

    def index(self, step, part, j):
        return part * (1 << self.steps) + (1 << step) - 1 + j

    def copy(self, step, part, j):
        i = self.index(step, part, j)
        return send(
            self.source(part, j),
            self.block(part, self.place(part, j)),
            self.sems.at[0, i],
            self.sems.at[1, i],
            self.device(self.orders[part][step] + 1),
        )

    def core_copy(self, part, j):
        i = part * (1 << self.steps) + j
        return send(
            self.source(part, j),
            self.block(part, self.place(part, j)),
            self.core_sems.at[0, i],
            self.core_sems.at[1, i],
            self.device(0),
        )

    def start(self):
        for part in range(3):
            for step in range(self.steps):
                self.copy(step, part, 0).start()
        for part in range(3):
            self.core_copy(part, 0).start()
        self.keep().start()

    def keep(self):
        return pltpu.make_async_copy(self.own, self.every.at[self.plane], self.core_sems.at[1, 3 << self.steps])

    def next(self, step):
        for part in range(3):
            for j in range(1 << step):
                k = (1 << step) + j
                arrived(self.block(part, self.place(part, k)), self.sems.at[1, self.index(step, part, j)])
                for later in range(step + 1, self.steps):
                    self.copy(later, part, k).start()
                self.core_copy(part, k).start()

    def finish_in(self):
        for part in range(3):
            for j in range(1 << self.steps):
                there = self.block(part, flipped(self.place(part, j), 0))
                arrived(there, self.core_sems.at[1, part * (1 << self.steps) + j])
        self.keep().wait()

    def finish_out(self):
        for part in range(3):
            for j in range(1 << self.steps):
                self.core_copy(part, j).wait_send()
            for step in range(self.steps):
                for j in range(1 << step):
                    self.copy(step, part, j).wait_send()


class Halving:
    def __init__(self, at, bufs, sems, orders):
        self.at, self.bufs, self.sems = at, bufs, sems
        self.plane = at.quad * at.exps + at.exp
        self.places = bits_of(QUAD * at.exps)
        self.chip_bits = list(range(self.places - 1))
        self.parts = column_parts(bufs[0].shape[2])
        self.orders = orders

    def device(self, bit):
        other = flipped(self.plane, bit)
        return (self.at.grp, other // self.at.exps, other % self.at.exps)

    def hop(self, step, part):
        order = self.orders[part]
        bit = order[step]
        left = [b for b in self.chip_bits if b not in order[:step]]
        pos = left.index(bit)
        half = 1 << (len(left) - 1)
        mine = (self.plane // (1 << (bit + 1))) % 2
        device = self.device(bit + 1)
        begin, size = self.parts[part]
        cols = pl.ds(begin, size)
        base = self.base(step, part)

        def index(j, value):
            return (j >> pos) * (1 << (pos + 1)) + value * (1 << pos) + j % (1 << pos)

        pairs = []
        for j in range(half):
            copy = functools.partial(
                send,
                self.bufs[step].at[index(j, 1 - mine), :, cols],
                self.bufs[step + 1].at[j, :, cols],
                self.sems.at[0, base + j],
                self.sems.at[1, base + j],
                device,
            )
            pairs.append((copy, index(j, mine), j))
        return pairs, begin, size, base

    def base(self, step, part):
        n = len(self.chip_bits)
        return part * (1 << n) + sum(1 << (n - 1 - s) for s in range(step))

    def start(self, step, part=None):
        for p in range(3) if part is None else [part]:
            for copy, _, _ in self.hop(step, p)[0]:
                copy().start()

    def add(self, step, part):
        pairs, begin, size, base = self.hop(step, part)
        cols = pl.ds(begin, size)
        here, there = self.bufs[step], self.bufs[step + 1]
        for _, keep, j in pairs:
            arrived(there.at[j, :, cols], self.sems.at[1, base + j])
            there[j, :, begin : begin + size] = (
                there[j, :, begin : begin + size] + here[keep, :, begin : begin + size]
            )

    def next(self, step):
        for p in range(3):
            self.add(step, p)
            if step + 1 < len(self.chip_bits):
                self.start(step + 1, p)

    def result(self):
        return self.bufs[len(self.chip_bits)]

    def finish(self):
        for step in range(len(self.chip_bits)):
            for p in range(3):
                for copy, _, _ in self.hop(step, p)[0]:
                    copy().wait_send()


class Group:
    def __init__(self, at, own, every, sems):
        self.at, self.own, self.every, self.sems = at, own, every, sems
        self.beside, self.across = at.exp + 1 - 2 * (at.exp % 2), (at.exp + 2) % 4

    def copy(self, src, index, send_index, device):
        return send(
            src, self.every.at[index], self.sems.at[0, send_index], self.sems.at[1, index], self.at.device(self.at.rep, device)
        )

    def first(self):
        return [
            self.copy(self.own, self.at.exp, 0, self.across),
            self.copy(self.own, self.at.exp, 1, self.beside),
        ]

    def second(self):
        return self.copy(self.every.at[self.across], self.across, 2, self.beside)

    def start(self):
        for copy in self.first():
            copy.start()

    def pass_on(self):
        arrived(self.every.at[self.across], self.sems.at[1, self.across])
        self.second().start()

    def arrive(self):
        for index in (self.beside, (self.beside + 2) % 4):
            arrived(self.every.at[index], self.sems.at[1, index])

    def sent(self):
        for copy in self.first() + [self.second()]:
            copy.wait_send()


class Tiles:
    def __init__(self, units, reps):
        self.units = units
        self.reps = reps
        self.hidden = units * reps
        self.half = self.hidden // 256
        self.wide = (self.half + 1) // 2
        self.count = 3
        self.size = 128 * self.wide // self.count
        self.skip = 128 * (2 * self.wide - self.half)

    def start(self, quad):
        return 128 * (self.half * (quad // 2) + (self.half - self.wide) * (quad % 2))

    def rows(self, tile):
        result = []
        for k in range(QUAD):
            found = None
            for parity in range(2):
                first = self.start(parity) + tile * self.size
                live = first + (self.skip if parity and tile == 0 else 0)
                begin = max(live, k * self.units)
                end = min(first + self.size, (k + 1) * self.units)
                if end > begin:
                    found = (begin - k * self.units, end - begin, parity, begin - first)
            result.append(found)
        return result


class Outward:
    def __init__(self, at, tiles, tile, in_low, down_slab, both_w, down_w, nothing, sems, down_sems):
        self.at, self.tiles, self.tile = at, tiles, tile
        self.in_low, self.down_slab, self.both_w, self.down_w = in_low, down_slab, both_w, down_w
        self.nothing, self.sems, self.down_sems = nothing, sems, down_sems
        self.slab = in_low.shape[0]

    def source(self, quad, section):
        begin = section * self.tiles.hidden + self.tiles.start(quad) + self.tile * self.tiles.size
        return self.in_low.at[:, pl.ds(pl.multiple_of(begin, 128), self.tiles.size)]

    def target(self, rep, section):
        rows = pl.ds(pl.multiple_of(rep * self.slab, self.slab), self.slab)
        return self.both_w.at[rows, pl.ds(section * self.tiles.size, self.tiles.size)]

    def over(self, act, first=1, last=None):
        at = self.at

        def one(k, _):
            other = (at.rep + k) % at.reps
            for section in range(2):
                act(
                    functools.partial(
                        send,
                        self.source(other % QUAD, section),
                        self.target(at.rep, section),
                        self.sems.at[0, section * at.reps + other],
                        self.sems.at[1, section * at.reps + at.rep],
                        at.device(other, at.exp),
                    )
                )
            return 0

        lax.fori_loop(first, last or at.reps, one, 0)

    def over_down(self, act, act_local):
        at = self.at
        for k, piece in enumerate(self.tiles.rows(self.tile)):
            if piece is None:
                continue
            begin, count, parity, to = piece
            quad = 2 * (at.rep // QUAD) + parity
            src, dst = self.down_slab.at[pl.ds(begin, count)], self.down_w.at[pl.ds(to, count)]
            recv = self.down_sems.at[1, at.rep]
            for g in range(at.grps):
                stays = jnp.logical_and(at.grp == g, at.quad == quad)
                ours = at.rep % QUAD == k

                @pl.when(jnp.logical_and(ours, jnp.logical_not(stays)))
                def _():
                    act(functools.partial(send, src, dst, self.down_sems.at[0, g], recv, (g, quad, at.exp)))

                @pl.when(jnp.logical_and(ours, stays))
                def _():
                    act_local(functools.partial(pltpu.make_async_copy, src, dst, recv))

    def blank(self):
        return pltpu.make_async_copy(
            self.nothing, self.down_w.at[pl.ds(0, self.tiles.skip)], self.down_sems.at[1, self.at.reps]
        )

    def start(self, first=1, last=None):
        at = self.at
        self.over(lambda copy: copy().start(), first, last)
        if first > 1:
            return
        self.over_down(lambda copy: copy().start(), lambda copy: copy().start())
        for section in range(2):
            pltpu.make_async_copy(
                self.source(at.quad, section), self.target(at.rep, section), self.sems.at[1, section * at.reps + at.rep]
            ).start()
        if self.tile == 0:

            @pl.when(at.quad % 2 == 1)
            def _():
                self.blank().start()

    def arrive(self):
        at = self.at

        def one(rep, _):
            for section in range(2):
                arrived(self.target(rep, section), self.sems.at[1, section * at.reps + rep])
            return 0

        lax.fori_loop(0, at.reps, one, 0)
        for parity in range(2):

            @pl.when(at.quad % 2 == parity)
            def _():
                for k, piece in enumerate(self.tiles.rows(self.tile)):
                    if piece is not None and piece[2] == parity:
                        source = QUAD * (at.quad // 2) + k
                        arrived(self.down_w.at[pl.ds(piece[3], piece[1])], self.down_sems.at[1, source])
                if parity and self.tile == 0:
                    self.blank().wait()

    def sent(self):
        self.over(lambda copy: copy().wait_send())
        self.over_down(lambda copy: copy().wait_send(), lambda copy: None)


class Homeward:
    def __init__(self, at, tiles, tile, both, down, in_parts, down_parts, sems, down_sems, sections=(0, 1)):
        self.at, self.tiles, self.tile, self.sections = at, tiles, tile, sections
        self.both, self.down, self.in_parts, self.down_parts = both, down, in_parts, down_parts
        self.sems, self.down_sems = sems, down_sems
        self.slab = in_parts.shape[1]

    def target(self, grp, quad, parity, section):
        skip = self.tiles.skip if parity and self.tile == 0 else 0
        to = section * self.tiles.hidden + self.tiles.start(quad) + self.tile * self.tiles.size + skip
        to = to if isinstance(to, int) else pl.multiple_of(to, 128)
        return skip, self.in_parts.at[grp, :, pl.ds(to, self.tiles.size - skip)]

    def copy(self, rep, parity, section, local=False):
        at = self.at
        skip, dst = self.target(at.grp, at.quad, parity, section)
        rows = pl.ds(pl.multiple_of(rep * self.slab, self.slab), self.slab)
        src = self.both.at[rows, pl.ds(section * self.tiles.size + skip, self.tiles.size - skip)]
        recv = self.sems.at[1, section * at.reps + at.rep]
        if local:
            return pltpu.make_async_copy(src, dst, recv)
        return send(src, dst, self.sems.at[0, section * at.reps + rep], recv, at.device(rep, at.exp))

    def over(self, act, act_local):
        at = self.at
        for parity in range(2):

            @pl.when(at.quad % 2 == parity)
            def _():
                def one(k, _):
                    for section in self.sections:
                        act(self.copy((at.rep + k) % at.reps, parity, section))
                    return 0

                lax.fori_loop(1, at.reps, one, 0)
                if act_local:
                    for section in self.sections:
                        act_local(self.copy(at.rep, parity, section, local=True))

    def over_down(self, act, act_local):
        at = self.at
        if self.down is None:
            return
        for k, piece in enumerate(self.tiles.rows(self.tile)):
            if piece is None:
                continue
            begin, count, parity, to = piece
            src, dst = self.down.at[pl.ds(to, count)], self.down_parts.at[at.grp, pl.ds(begin, count)]
            recv = self.down_sems.at[1, at.grp]
            stays = jnp.logical_and(at.grp == at.quad // 2, at.quad == k)
            ours = at.quad % 2 == parity

            @pl.when(jnp.logical_and(ours, jnp.logical_not(stays)))
            def _():
                act(functools.partial(send, src, dst, self.down_sems.at[0, k], recv, (at.quad // 2, k, at.exp)))

            @pl.when(jnp.logical_and(ours, stays))
            def _():
                act_local(functools.partial(pltpu.make_async_copy, src, dst, recv))

    def start(self):
        self.over_down(lambda copy: copy().start(), lambda copy: copy().start())
        self.over(lambda copy: copy.start(), lambda copy: copy.start())

    def arrive(self):
        at = self.at
        for rep in range(at.reps):
            for section in self.sections:
                _, dst = self.target(rep // QUAD, rep % QUAD, rep % 2, section)
                arrived(dst, self.sems.at[1, section * at.reps + rep])
        for k, piece in enumerate(self.tiles.rows(self.tile)):
            if piece is None or self.down is None:
                continue

            @pl.when(at.quad == k)
            def _():
                for g in range(at.grps):
                    arrived(self.down_parts.at[g, pl.ds(piece[0], piece[1])], self.down_sems.at[1, g])

    def sent(self):
        self.over(lambda copy: copy.wait_send(), None)
        self.over_down(lambda copy: copy().wait_send(), lambda copy: None)


def forward_kernel(
    grps,
    exps,
    lengths,
    bias_table,
    routes_t,
    tokens,
    cotangent,
    gains,
    router,
    attn_qkv,
    attn_out,
    expert_in,
    expert_out,
    both_w,
    down_w,
    cot_all,
    n_all,
    comb_all,
    qkv_out,
    pb_out,
    mine_out,
    n1_out,
    wqkv_out,
    wout_out,
    h1_out,
    n2_out,
    probs_out,
    in_out,
    down_out,
    in_wide,
    down_wide,
    qkv_t,
    out_w,
    in_low,
    down_slab,
    tok_all,
    wqkv,
    wout,
    n1,
    qkv,
    pb,
    mine,
    ctx,
    bias,
    comb_send,
    nothing,
    tok_sem,
    wq_sem,
    wo_sem,
    wo2_sem,
    weight_sem,
    down_sem,
    ctx_sem,
    cot_sem,
    cot_core_sem,
    n_sem,
    n_core_sem,
    comb_sem,
    store_sem,
    cast_sem,
):
    at = Where(grps, exps)
    reps = at.reps
    rows, width = tokens.shape
    heads = HEADS // exps
    head_dim = width // HEADS
    head_cols = heads * head_dim
    block_cols = min(128, head_cols)
    shard_cols, row_block = qkv_t.shape
    seg = math.gcd(shard_cols, head_cols)
    segs = shard_cols // seg
    tiles = Tiles(down_slab.shape[0], reps)
    plane = at.quad * exps + at.exp
    members = QUAD * exps
    scale = 1.0 / math.sqrt(head_dim)
    SEND, RECV = 0, 1

    met = greet(*everyone(at))
    wide_copies = [
        pltpu.make_async_copy(expert_in, in_wide, cast_sem.at[0]),
        pltpu.make_async_copy(expert_out, down_wide, cast_sem.at[1]),
    ]
    for copy in wide_copies:
        copy.start()
    qkv_t[...] = attn_qkv[...].T.astype(low)
    out_w[...] = attn_out[...].astype(low)
    met()

    def exp_peer(k):
        return (at.exp + k) % exps

    group_tokens = Group(at, tokens, tok_all, tok_sem)
    group_tokens.start()
    tok_all[at.exp] = tokens[...]

    def segment(k):
        col = (at.rep * segs + k) * seg
        section = col // width
        within = col - section * width
        owner = within // head_cols
        return owner, section * head_cols + within - owner * head_cols

    def segment_copy(k, shift):
        owner, offset = segment(k)
        src = qkv_t.at[pl.ds(k * seg, seg)]
        dst = wqkv.at[at.exp, pl.ds(pl.multiple_of(offset, seg), seg)]
        target = at.device((at.rep + shift) % reps, owner)
        return owner, src, dst, functools.partial(
            send, src, dst, wq_sem.at[SEND, k * reps + shift], wq_sem.at[RECV, at.exp * 3 * (head_cols // seg) + offset // seg], target
        )

    def over_segments(act, act_local):
        def one(i, _):
            k, shift = i // reps, i % reps
            owner, src, dst, copy = segment_copy(k, shift)
            stays = jnp.logical_and(shift == 0, owner == at.exp)

            @pl.when(jnp.logical_not(stays))
            def _():
                act(copy())

            @pl.when(stays)
            def _():
                act_local(k, src, dst)

            return 0

        lax.fori_loop(0, segs * reps, one, 0)

    def local_segment(k, src, dst):
        _, offset = segment(k)
        pltpu.make_async_copy(src, dst, wq_sem.at[RECV, at.exp * 3 * (head_cols // seg) + offset // seg]).start()

    over_segments(lambda copy: copy.start(), local_segment)

    for k in range(1, reps):
        other = (at.rep + k) % reps
        send(
            out_w, wout.at[at.exp, at.rep], wo_sem.at[SEND, other], wo_sem.at[RECV, at.rep], at.device(other, at.exp)
        ).start()
    wout[at.exp, at.rep] = out_w[...]
    chip_bits = list(range(bits_of(members) - 1))
    cots = Doubling(at, cotangent, cot_all, cot_sem, cot_core_sem, [chip_bits[::-1]] * 3)
    cots.start()

    span = 2 * rows
    bucket = bucket_of(lane_of((8, span)) - rows)
    for h in range(heads):
        line = jnp.zeros((8, span), full)
        for b in range(BUCKETS):
            line = jnp.where(bucket == b, bias_table[at.exp * heads + h, b], line)
        whole = jnp.broadcast_to(line[0:1], (rows, span))
        bias[h] = pltpu.roll(whole, 0, 1, stride=1, stride_axis=0)[:, rows:]

    group_tokens.pass_on()
    group_tokens.arrive()

    def norm_group(s, _):
        x = tok_all[s].astype(full)
        r = lax.rsqrt(jnp.mean(x * x, axis=1, keepdims=True) + eps_norm)
        n1[s] = (x * r * gains[0:1, :]).astype(low)
        return 0

    lax.fori_loop(0, exps, norm_group, 0)

    for copy in wide_copies:
        copy.wait()
    in_low[...] = in_wide[...].astype(low)
    down_slab[...] = down_wide[...].astype(low)
    nothing[...] = jnp.zeros_like(nothing)
    weights = [
        Outward(
            at, tiles, t, in_low, down_slab, both_w.at[t], down_w.at[t], nothing, weight_sem.at[t], down_sem.at[t]
        )
        for t in range(2)
    ]

    weights[0].start()

    def wait_segment(i, _):
        e, j = i // (3 * head_cols // seg), i % (3 * head_cols // seg)
        arrived(wqkv.at[e, pl.ds(pl.multiple_of(j * seg, seg), seg)], wq_sem.at[RECV, i])
        return 0

    lax.fori_loop(0, exps * 3 * head_cols // seg, wait_segment, 0)

    def project(s, _):
        total = jnp.zeros((rows, 3 * head_cols), full)
        for e in range(exps):
            total = total + nt(n1[s, :, e * row_block : (e + 1) * row_block], wqkv[e])
        qkv[s] = total.astype(low)
        return 0

    lax.fori_loop(0, exps, project, 0)

    group_wout = Group(at, wout.at[at.exp], wout, wo2_sem)

    def beside(k):
        if k == 1:
            for j in range(1, reps):
                other = (at.rep + j) % reps
                arrived(wout.at[at.exp, other], wo_sem.at[RECV, other])
            group_wout.start()
        elif k == 2:
            cots.next(0)
        else:
            group_wout.pass_on()

    def attend(i, _):
        s = turn(at.exp, i)
        for k in range(1, exps):

            @pl.when(i == k)
            def _():
                beside(k)

        ok = lane_of((rows, rows)) < lengths[at.base + s]
        lane = lane_of((rows, block_cols))
        for c in range(head_cols // block_cols):
            cols = slice(c * block_cols, (c + 1) * block_cols)
            q = qkv[s, :, cols] * scale
            k = qkv[s, :, head_cols + c * block_cols : head_cols + (c + 1) * block_cols]
            v = qkv[s, :, 2 * head_cols + c * block_cols : 2 * head_cols + (c + 1) * block_cols]
            result = jnp.zeros((rows, block_cols), full)
            for t in range(block_cols // head_dim):
                h = c * (block_cols // head_dim) + t
                here = jnp.logical_and(lane >= t * head_dim, lane < (t + 1) * head_dim)
                scores = nt(jnp.where(here, q, jnp.zeros_like(q)), k) + bias[h]
                scores = jnp.where(ok, scores, -1e30)
                top = jnp.max(scores, axis=1, keepdims=True)
                weights = jnp.exp(scores - top)
                total = jnp.sum(weights, axis=1, keepdims=True)
                weights = (weights * (1.0 / total)).astype(low)
                result = jnp.where(here, jnp.dot(weights, v, preferred_element_type=full), result)
                pb[s * heads + h] = weights
            mine[s, :, cols] = result.astype(low)

        @pl.when(i < exps - 1)
        def _():
            send(
                mine.at[s], ctx.at[at.exp], ctx_sem.at[SEND, s], ctx_sem.at[RECV, at.exp], at.device(at.rep, s)
            ).start()

        @pl.when(i == exps - 1)
        def _():
            pltpu.make_async_copy(mine.at[s], ctx.at[at.exp], ctx_sem.at[RECV, at.exp]).start()

        return 0

    lax.fori_loop(0, exps, attend, 0)

    cots.next(1)
    group_wout.arrive()
    for e in range(exps):
        arrived(ctx.at[e], ctx_sem.at[RECV, e])

    out_cols = wout.shape[3]
    for r in range(reps):
        cols = slice(r * out_cols, (r + 1) * out_cols)
        total = tokens[:, cols].astype(full)
        for e in range(exps):
            total = total + jnp.dot(ctx[e], wout[e, r], preferred_element_type=full)
        h1_out[:, cols] = total
    h1 = h1_out[...]
    r2 = lax.rsqrt(jnp.mean(h1 * h1, axis=1, keepdims=True) + eps_norm)
    n2 = (h1 * r2 * gains[1:2, :]).astype(low)
    n2_out[...] = n2
    rotated = [chip_bits[c:] + chip_bits[:c] for c in range(3)]
    rows_two = Doubling(at, n2_out, n_all, n_sem, n_core_sem, rotated)
    rows_two.start()
    weights[1].start(1, 3)

    router_rows = jnp.concatenate([router[...], jnp.zeros((128 - exps, width), full)], axis=0)
    logits = nt(n2.astype(full), router_rows, precision=highest)
    lane = lane_of((rows, 128))
    logits = jnp.where(lane < exps, logits, -1e30)
    probs = jnp.exp(logits - jnp.max(logits, axis=1, keepdims=True))
    probs = probs / jnp.sum(probs, axis=1, keepdims=True)
    probs_out[...] = probs
    picked = jnp.where(routed(routes_t, at.me, rows), probs, 0.0)
    comb = picked / jnp.sum(picked, axis=1, keepdims=True)
    comb = jnp.where(row_of((rows, 1)) < lengths[at.me], comb, 0.0)
    comb_send[...] = comb.T[0 : comb_send.shape[0]]

    def comb_copy(k):
        other = (plane + k) % members
        return send(
            comb_send,
            comb_all.at[plane],
            comb_sem.at[SEND, other],
            comb_sem.at[RECV, plane],
            (at.grp, other // exps, other % exps),
        )

    def start_comb(k, _):
        comb_copy(k).start()
        return 0

    lax.fori_loop(1, members, start_comb, 0)
    pltpu.make_async_copy(comb_send, comb_all.at[plane], comb_sem.at[RECV, plane]).start()
    rows_two.next(0)
    weights[1].start(3, 5)

    stores = [
        (qkv, qkv_out),
        (pb, pb_out),
        (mine, mine_out),
        (n1, n1_out),
        (wqkv, wqkv_out),
        (wout, wout_out),
        (in_low, in_out),
        (down_slab, down_out),
    ]
    for i, (src, dst) in enumerate(stores):
        pltpu.make_async_copy(src, dst, store_sem.at[i]).start()

    rows_two.next(1)
    weights[1].start(5)
    for step in range(2, rows_two.steps):
        rows_two.next(step)
    for step in range(2, cots.steps):
        cots.next(step)

    cots.finish_in()
    rows_two.finish_in()

    def comb_in(k, _):
        arrived(comb_all.at[k], comb_sem.at[RECV, k])
        return 0

    lax.fori_loop(0, members, comb_in, 0)
    for tile in weights:
        tile.arrive()

    for k in range(1, exps):
        peer = exp_peer(k)
        arrived(mine.at[peer], ctx_sem.at[SEND, peer])
    over_segments(lambda copy: copy.wait_send(), lambda k, src, dst: None)
    for k in range(1, reps):
        arrived(out_w, wo_sem.at[SEND, (at.rep + k) % reps])
    group_tokens.sent()
    group_wout.sent()
    cots.finish_out()
    rows_two.finish_out()

    def sent_comb(k, _):
        comb_copy(k).wait_send()
        return 0

    lax.fori_loop(1, members, sent_comb, 0)
    for tile in weights:
        tile.sent()
    for i, (src, dst) in enumerate(stores):
        pltpu.make_async_copy(src, dst, store_sem.at[i]).wait()


def forward_call(
    grps, exps, lengths, bias_table, routes_t, tokens, cotangent, gains, router, attn_qkv, attn_out, expert_in, expert_out
):
    reps = grps * QUAD
    rows, width = tokens.shape
    head_cols = width // exps
    row_block, shard_cols = attn_qkv.shape
    seg = math.gcd(shard_cols, head_cols)
    segs = shard_cols // seg
    units = expert_out.shape[0]
    out_cols = attn_out.shape[1]
    heads = HEADS // exps
    members = QUAD * exps
    tiles = Tiles(units, reps)
    shape = jax.ShapeDtypeStruct
    vmem = pl.BlockSpec(memory_space=pltpu.VMEM)
    smem = pl.BlockSpec(memory_space=pltpu.SMEM)
    hbm = pl.BlockSpec(memory_space=pl.ANY)
    results = [
        (shape((2, width, 2 * tiles.size), low), hbm),
        (shape((2, tiles.size, width), low), hbm),
        (shape((members, rows, width), low), hbm),
        (shape((members, rows, width), low), hbm),
        (shape((members, 8, rows), full), hbm),
        (shape((exps, rows, 3 * head_cols), low), hbm),
        (shape((exps * heads, rows, rows), low), hbm),
        (shape((exps, rows, head_cols), low), hbm),
        (shape((exps, rows, width), low), hbm),
        (shape((exps, 3 * head_cols, row_block), low), hbm),
        (shape((exps, reps, row_block, out_cols), low), hbm),
        (shape((rows, width), full), vmem),
        (shape((rows, width), low), vmem),
        (shape((rows, 128), full), vmem),
        (shape(expert_in.shape, low), hbm),
        (shape(expert_out.shape, low), hbm),
    ]
    dma = pltpu.SemaphoreType.DMA
    chips = members // 2
    return pl.pallas_call(
        functools.partial(forward_kernel, grps, exps),
        out_shape=[r[0] for r in results],
        in_specs=[smem] * 2 + [vmem] * 7 + [hbm] * 2,
        out_specs=[r[1] for r in results],
        scratch_shapes=[
            pltpu.VMEM(expert_in.shape, full),
            pltpu.VMEM(expert_out.shape, full),
            pltpu.VMEM((shard_cols, row_block), low),
            pltpu.VMEM((row_block, out_cols), low),
            pltpu.VMEM(expert_in.shape, low),
            pltpu.VMEM(expert_out.shape, low),
            pltpu.VMEM((exps, rows, width), low),
            pltpu.VMEM((exps, 3 * head_cols, row_block), low),
            pltpu.VMEM((exps, reps, row_block, out_cols), low),
            pltpu.VMEM((exps, rows, width), low),
            pltpu.VMEM((exps, rows, 3 * head_cols), low),
            pltpu.VMEM((exps * heads, rows, rows), low),
            pltpu.VMEM((exps, rows, head_cols), low),
            pltpu.VMEM((exps, rows, head_cols), low),
            pltpu.VMEM((heads, rows, rows), full),
            pltpu.VMEM((8, rows), full),
            pltpu.VMEM((tiles.skip, width), low),
            dma((2, exps)),
            dma((2, max(segs * reps, exps * 3 * head_cols // seg))),
            dma((2, reps)),
            dma((2, exps)),
            dma((2, 2, 2 * reps)),
            dma((2, 2, reps + 1)),
            dma((2, exps)),
            dma((2, 3 * chips)),
            dma((2, 3 * chips + 1)),
            dma((2, 3 * chips)),
            dma((2, 3 * chips + 1)),
            dma((2, members)),
            dma((8,)),
            dma((2,)),
        ],
        compiler_params=pltpu.CompilerParams(
            collective_id=0, has_side_effects=True, vmem_limit_bytes=60 * 1024 * 1024
        ),
        name="forward",
    )(lengths, bias_table, routes_t, tokens, cotangent, gains, router, attn_qkv, attn_out, expert_in, expert_out)


def expert_kernel(
    grps,
    exps,
    cap,
    deal,
    routes_t,
    comb,
    n_all,
    cot_all,
    both_w,
    down_w,
    in_low,
    down_slab,
    h1,
    n_total,
    y_half,
    y_far,
    c_in,
    both_g,
    down_g,
    in_parts,
    down_parts,
    place,
    marks,
    n_rows,
    g_rows,
    both_v,
    down_v,
    raw_n,
    raw_g,
    y_acc,
    n_acc,
    both_d,
    active,
    n_bufs,
    c_sum,
    out_y,
    load_sem,
    raw_sem,
    out_sem,
    in_sem,
    in_down_sem,
    home_sem,
    home_down_sem,
    stage_sem,
    far_sem,
    n_sem,
    c_sem,
):
    at = Where(grps, exps)
    rows, width = n_all.shape[1:]
    tiles = Tiles(down_slab.shape[0], at.reps)
    size = tiles.size
    slots = exps * cap
    members = QUAD * exps
    loads = [pltpu.make_async_copy(both_w.at[t], both_v.at[t], load_sem.at[0, t]) for t in range(2)] + [
        pltpu.make_async_copy(down_w.at[t], down_v.at[t], load_sem.at[1, t]) for t in range(2)
    ]
    for copy in loads:
        copy.start()

    def raw_copies(q):
        here = pl.ds(pl.multiple_of(q * exps, exps), exps)
        return [
            pltpu.make_async_copy(n_all.at[here], raw_n.at[pl.ds(q % 2 * exps, exps)], raw_sem.at[0, q % 2]),
            pltpu.make_async_copy(cot_all.at[here], raw_g.at[pl.ds(q % 2 * exps, exps)], raw_sem.at[1, q % 2]),
        ]

    for copy in raw_copies(0):
        copy.start()

    beside = at.exp + 1 - 2 * (at.exp % 2)
    greet(*neighbours(at))()
    last = tiles.count - 1
    incoming = Outward(
        at, tiles, last, in_low, down_slab, both_v.at[last], down_v.at[last], None, in_sem, in_down_sem
    )
    incoming.start()
    home = Homeward(
        at, tiles, 0, both_v.at[0], down_v.at[0], in_parts, down_parts, home_sem, home_down_sem
    )

    earlier = jnp.where(row_of((rows, rows)) < lane_of((rows, rows)), 1.0, 0.0).astype(low)
    slot = row_of((cap, rows)).astype(full)

    def dispatch(q, _):
        @pl.when(q + 1 < QUAD)
        def _():
            for copy in raw_copies(q + 1):
                copy.start()

        for copy in raw_copies(q):
            copy.wait()
        lines = []
        for j in range(exps):
            seq = at.grp * members + q * exps + j
            pair = routes_t[:, pl.ds(pl.multiple_of(seq * rows, rows), rows)]
            lines.append(jnp.logical_or(pair[0:1] == at.exp, pair[1:2] == at.exp))
        lines = [jnp.where(line, 1.0, 0.0) for line in lines] + [jnp.zeros((8 - exps, rows), full)]
        hot_low = jnp.concatenate(lines, axis=0).astype(low)
        before = dot(hot_low, earlier)
        for j in range(exps):
            s = q * exps + j
            inside = jnp.logical_and(slot == before[j : j + 1, :], hot_low[j : j + 1, :].astype(full) > 0.5)
            here = jnp.where(inside, 1.0, 0.0)
            place[s] = here.astype(low)
            g = raw_g[q % 2 * exps]
            for b in range(1, exps):
                g = jnp.where(deal[at.grp * members + s] == at.grp * members + q * exps + b, raw_g[q % 2 * exps + b], g)
            where = pl.ds(pl.multiple_of(s * cap, cap), cap)
            n_rows[where] = dot(here.astype(low), raw_n[q % 2 * exps + j]).astype(low)
            g_rows[where] = dot(here.astype(low), g).astype(low)
            marks[where, 0:1] = jnp.sum(here * comb[s, pl.ds(at.exp, 1), :], axis=1, keepdims=True)
            marks[where, 1:2] = jnp.zeros((cap, 1), full)
        return 0

    lax.fori_loop(0, QUAD, dispatch, 0)
    for copy in loads:
        copy.wait()
    curve = math.sqrt(2.0 / math.pi)

    core = at.exp % 2

    plane = at.quad * exps + at.exp
    sibling = at.device(at.rep, beside)
    dn = Halving(at, n_bufs, n_sem, [[0, 1, 2], [1, 2, 0], [2, 0, 1]])

    def n_copy(j):
        return send(raw_n.at[j], n_bufs[0].at[j], far_sem.at[0, 0, j], far_sem.at[0, 1, j], sibling)

    def y_copies(j):
        return (
            pltpu.make_async_copy(out_y.at[j % 2], y_half.at[j], out_sem.at[j % 2]),
            send(raw_n.at[j], y_far.at[j], far_sem.at[1, 0, j], far_sem.at[1, 1, j], sibling),
        )

    def c_copy(k):
        other = (plane + k) % members
        return send(
            c_sum.at[other],
            c_in.at[plane],
            c_sem.at[0, other],
            c_sem.at[1, plane],
            (at.grp, other // exps, other % exps),
        )

    def slots_of(s):
        return pl.ds(pl.multiple_of(s * cap, cap), cap)

    def n_rows_of(s):
        where = slots_of(s)
        line = jnp.sum(place[s].astype(full) * marks[where, 1:2], axis=0, keepdims=True)
        c_sum[s] = jnp.broadcast_to(line, (8, rows))
        return tn(place[s], n_acc[where]).astype(low)

    def y_rows_of(p):
        first = p // exps * exps
        spot = at.grp * members + p
        here, y = place[first], y_acc[slots_of(first)]
        for c in range(1, exps):
            taken = deal[at.grp * members + first + c] == spot
            here = jnp.where(taken, place[first + c], here)
            y = jnp.where(taken, y_acc[slots_of(first + c)], y)
        return (tn(here, y) + jnp.where(deal[at.me] == spot, h1[...], 0.0)).astype(low)

    def give_n(j):
        raw_n[j] = n_rows_of(2 * j + 1 - core)
        n_copy(j).start()
        raw_g[j] = n_rows_of(2 * j + core)

    def add_n(quad):
        for k in range(exps // 2):
            j = quad * (exps // 2) + k
            arrived(n_bufs[0].at[j], far_sem.at[0, 1, j])
            n_bufs[0][j] = n_bufs[0][j] + raw_g[j]

    def give_y(j, _):
        @pl.when(j >= 2)
        def _():
            y_copies(j - 2)[0].wait()

        out_y[j % 2] = y_rows_of(2 * j + core)
        n_copy(j).wait_send()
        raw_n[j] = y_rows_of(2 * j + 1 - core)
        for copy in y_copies(j):
            copy.start()
        return 0

    def start_c(k, _):
        c_copy(k).start()
        return 0

    def tile_work(f, _):
        @pl.when(f == last)
        def _():
            incoming.arrive()
            home.start()

        def chunk(i, _):
            c = jnp.where(i == 0, at.near(3), jnp.where(i == 1, at.near(1), jnp.where(i == 2, at.near(2), at.quad)))
            here = pl.ds(pl.multiple_of(c * slots, slots), slots)
            share = marks[here, 0:1]
            both = dot(n_rows[here], both_v[f])
            gate_part, up_part = both[:, :size], both[:, size:]
            grad = nt(g_rows[here], down_v[f])
            square = gate_part * gate_part
            bend = jnp.tanh(curve * gate_part * (1.0 + 0.044715 * square))
            half = 0.5 * (1.0 + bend)
            gelu = gate_part * half
            slope = half + (0.5 * curve) * gate_part * (1.0 - bend * bend) * (1.0 + (3 * 0.044715) * square)
            value = gelu * up_part
            marks[here, 1:2] += jnp.sum(value * grad, axis=1, keepdims=True)
            grad = grad * share
            active[f % 2, here] = (value * share).astype(low)
            both_d[f % 2, here, :size] = (grad * up_part * slope).astype(low)
            both_d[f % 2, here, size:] = (grad * gelu).astype(low)
            y = dot(active[f % 2, here], down_v[f])
            y_acc[here] = jnp.where(f == 0, y, y_acc[here].astype(full) + y).astype(low)
            n_back = nt(both_d[f % 2, here], both_v[f])
            n_acc[here] = jnp.where(f == 0, n_back, n_acc[here].astype(full) + n_back).astype(low)

            @pl.when(f == last)
            def _():
                for k in range(exps // 2):
                    give_n(c * (exps // 2) + k)

            @pl.when(jnp.logical_and(f == last, i == 2))
            def _():
                add_n(at.near(3))

            @pl.when(jnp.logical_and(f == last, i == 3))
            def _():
                add_n(at.near(1))
                dn.start(0, 1)

            return 0

        lax.fori_loop(0, QUAD, chunk, 0)

        @pl.when(f == 0)
        def _():
            weight_work(0)

        return 0

    def weight_work(f):
        def columns(m, _):
            cols = pl.ds(pl.multiple_of(m * (width // 2), width // 2), width // 2)
            both_v[f, cols] = tn(n_rows[:, cols], both_d[f % 2]).astype(low)
            down_v[f, :, cols] = tn(active[f % 2], g_rows[:, cols]).astype(low)
            return 0

        lax.fori_loop(0, 2, columns, 0)

        for copy in stage_copies(f):
            copy.start()

    def stage_copies(f):
        if f == 0:
            return []
        return [
            pltpu.make_async_copy(both_v.at[f], both_g.at[f - 1], stage_sem.at[0, f]),
            pltpu.make_async_copy(down_v.at[f], down_g.at[f - 1], stage_sem.at[1, f]),
        ]

    lax.fori_loop(0, tiles.count, tile_work, 0)

    half = members // 2
    add_n(at.near(2))
    dn.start(0, 2)
    add_n(at.quad)
    dn.start(0, 0)
    lax.fori_loop(1, members, start_c, 0)
    c_in[plane] = c_sum[plane]
    weight_work(1)
    weight_work(2)
    dn.next(0)
    lax.fori_loop(0, half, give_y, 0)
    for step in range(1, len(dn.chip_bits)):
        dn.next(step)
    n_total[...] = dn.result()[0]
    for j in (half - 2, half - 1):
        y_copies(j)[0].wait()
    for f in range(tiles.count):
        for copy in stage_copies(f):
            copy.wait()

    def core_in(j, _):
        y_copies(j)[1].wait_send()
        arrived(y_far.at[j], far_sem.at[1, 1, j])
        return 0

    lax.fori_loop(0, half, core_in, 0)

    def c_done(k, _):
        c_copy(k).wait_send()
        other = (plane + k) % members
        arrived(c_in.at[other], c_sem.at[1, other])
        return 0

    lax.fori_loop(1, members, c_done, 0)
    dn.finish()
    home.arrive()
    incoming.sent()
    home.sent()


def expert_call(grps, exps, cap, deal, routes_t, comb_all, n_all, cot_all, both_w, down_w, in_low, down_slab, h1):
    members, rows, width = n_all.shape
    reps = grps * QUAD
    tiles = Tiles(down_slab.shape[0], reps)
    size = tiles.size
    slab, both_hidden = in_low.shape
    units = down_slab.shape[0]
    slots = exps * cap
    chip_bits = bits_of(members) - 1
    shape = jax.ShapeDtypeStruct
    vmem = pl.BlockSpec(memory_space=pltpu.VMEM)
    smem = pl.BlockSpec(memory_space=pltpu.SMEM)
    hbm = pl.BlockSpec(memory_space=pl.ANY)
    results = [
        (shape((rows, width), low), vmem),
        (shape((members // 2, rows, width), low), hbm),
        (shape((members // 2, rows, width), low), hbm),
        (shape((members, 8, rows), full), vmem),
        (shape((2, width, 2 * size), low), hbm),
        (shape((2, size, width), low), hbm),
        (shape((grps, slab, both_hidden), low), hbm),
        (shape((grps, units, width), low), hbm),
    ]
    dma = pltpu.SemaphoreType.DMA
    return pl.pallas_call(
        functools.partial(expert_kernel, grps, exps, cap),
        out_shape=[r[0] for r in results],
        in_specs=[smem] + [vmem] * 2 + [hbm] * 6 + [vmem],
        out_specs=[r[1] for r in results],
        scratch_shapes=[
            pltpu.VMEM((members, cap, rows), low),
            pltpu.VMEM((QUAD * slots, 128), full),
            pltpu.VMEM((QUAD * slots, width), low),
            pltpu.VMEM((QUAD * slots, width), low),
            pltpu.VMEM((tiles.count, width, 2 * size), low),
            pltpu.VMEM((tiles.count, size, width), low),
            pltpu.VMEM((2 * exps, rows, width), low),
            pltpu.VMEM((2 * exps, rows, width), low),
            pltpu.VMEM((QUAD * slots, width), low),
            pltpu.VMEM((QUAD * slots, width), low),
            pltpu.VMEM((2, QUAD * slots, 2 * size), low),
            pltpu.VMEM((2, QUAD * slots, size), low),
            [pltpu.VMEM((members >> (1 + step), rows, width), low) for step in range(chip_bits + 1)],
            pltpu.VMEM((members, 8, rows), full),
            pltpu.VMEM((2, rows, width), low),
            dma((2, 2)),
            dma((2, 2)),
            dma((2,)),
            dma((2, 2 * reps)),
            dma((2, reps + 1)),
            dma((2, 2 * reps)),
            dma((2, max(QUAD, grps))),
            dma((2, tiles.count)),
            dma((2, 2, members // 2)),
            dma((2, 3 << chip_bits)),
            dma((2, members)),
        ],
        compiler_params=pltpu.CompilerParams(
            collective_id=2, has_side_effects=True, vmem_limit_bytes=60 * 1024 * 1024
        ),
        name="experts",
    )(deal, routes_t, comb_all, n_all, cot_all, both_w, down_w, in_low, down_slab, h1)


def adamw_root(weight, moment, second, gradient, step_rate, decay_factor):
    new_moment = beta_one * moment + (1.0 - beta_one) * gradient
    new_second = beta_two * second + (1.0 - beta_two) * gradient * gradient
    root = lax.rsqrt(new_second * (1.0 / (1.0 - beta_two**STEP)))
    step = new_moment * (root * (1.0 - eps_adam * root))
    keep = 1.0 - step_rate * decay_factor
    return (new_moment, new_second, keep * weight - (step_rate / (1.0 - beta_one**STEP)) * step)


def adam_kernel(exps, *refs):
    in_parts, down_parts, qkv_grad, out_grad, small = refs[:5]
    states, news, bias_grad = refs[5:26], refs[26:47], refs[47]
    heads = HEADS // exps
    width = small.shape[1]

    def update(i, grad, rate, decay):
        weight, first, second = [state[...] for state in states[3 * i : 3 * i + 3]]
        values = adamw_root(weight, first, second, grad, rate, decay)
        for new, value in zip(news[3 * i : 3 * i + 3], values, strict=True):
            new[...] = value

    def total(parts):
        result = parts[0].astype(full)
        for k in range(1, parts.shape[0]):
            result = result + parts[k].astype(full)
        return result

    @pl.when(pl.program_id(0) == 0)
    def _():
        update(0, qkv_grad[...], 1.5 / math.sqrt(D), 0.1)
        update(1, out_grad[...], 6.0 / math.sqrt(D), 0.1)
        for e in range(exps):
            for h in range(heads):
                bias_grad[e * heads + h : e * heads + h + 1, :] = small[
                    exps + 3 + e : exps + 4 + e, h * 128 : h * 128 + BUCKETS
                ]
        update(2, bias_grad[...], 0.3, 0.0)
        update(3, small[0:exps, :], 1.0 / math.sqrt(D), 0.1)
        update(4, small[exps : exps + 2, :], 0.5, 0.0)

    update(5, total(in_parts), 1.5 / math.sqrt(D), 0.1)
    update(6, total(down_parts), 1.5 / math.sqrt(FF), 0.1)


def adam_call(exps, in_parts, down_parts, qkv_grad, out_grad, small, states):
    steps = 4

    def whole(array):
        return pl.BlockSpec(array.shape, lambda i: (0,) * array.ndim)

    def columns(array):
        block = array.shape[:-1] + (array.shape[-1] // steps,)
        return pl.BlockSpec(block, lambda i: (0,) * (array.ndim - 1) + (i,))

    specs = [whole(state) for state in states[:15]]
    specs += [columns(state) for state in states[15:18]] + [columns(state) for state in states[18:]]
    return pl.pallas_call(
        functools.partial(adam_kernel, exps),
        grid=(steps,),
        in_specs=[columns(in_parts), columns(down_parts), whole(qkv_grad), whole(out_grad), whole(small)] + specs,
        out_specs=specs,
        out_shape=[jax.ShapeDtypeStruct(state.shape, full) for state in states],
        scratch_shapes=[pltpu.VMEM((HEADS, BUCKETS), full)],
        compiler_params=pltpu.CompilerParams(vmem_limit_bytes=60 * 1024 * 1024),
        name="adam",
    )(in_parts, down_parts, qkv_grad, out_grad, small, *states)


def backward_kernel(
    grps,
    exps,
    lengths,
    deal,
    y_half,
    y_far,
    both_g,
    down_g,
    in_before,
    down_before,
    n1_in,
    cot_all,
    routes_t,
    tokens,
    n_total,
    c_in,
    n2_in,
    probs_in,
    h1_from,
    qkv_from,
    pb_from,
    mine_from,
    wqkv_from,
    wout_from,
    gains,
    router_t,
    *rest,
):
    token_grad, block_out, in_parts, down_parts, qkv_grad, out_grad, small_out = rest[:7]
    scratch = rest[7:]
    (
    h1_in,
    qkv,
    pb,
    mine,
    wqkv,
    wout,
    kept,
    y_bufs,
    dh1,
    dz_send,
    dz_all,
    do_send,
    do_in,
    bias_sum,
    dqkv,
    dqkv_t,
    dn1_send,
    dn1_in,
    wq_send,
    og_send,
    mids,
    far_send,
    far_in,
    small_send,
    small_exp,
    small_sum,
    small_rep,
    small_half,
    small_far,
    y_sem,
    load_sem,
    weight_sem,
    down_sem,
    dz_sem,
    do_sem,
    dn1_sem,
    wq_sem,
    og_sem,
    mid_sem,
    far_sem,
    small_sem,
    small2_sem,
    small3_sem,
    n1_sem,
    operand_sem,
    ) = scratch
    at = Where(grps, exps)
    reps = at.reps
    rows, width = tokens.shape
    heads = HEADS // exps
    head_dim = width // HEADS
    head_cols = heads * head_dim
    block_cols = min(128, head_cols)
    row_block = wqkv.shape[2]
    out_cols = wout.shape[3]
    tiles = Tiles(down_parts.shape[1], reps)
    scale = 1.0 / math.sqrt(head_dim)
    SEND, RECV = 0, 1
    plane = at.quad * exps + at.exp
    members = QUAD * exps

    def exp_peer(k):
        return (at.exp + k) % exps

    router = router_t[...]
    met = greet(*neighbours(at))
    n1 = kept.at[0:exps]
    group = pl.ds(pl.multiple_of(at.quad * exps, exps), exps)
    cot_copy = pltpu.make_async_copy(cot_all.at[group], dn1_send, n1_sem.at[1])
    cot_copy.start()
    loads = [
        pltpu.make_async_copy(src, dst, operand_sem.at[i])
        for i, (src, dst) in enumerate(
            ((h1_from, h1_in), (wout_from, wout), (qkv_from, qkv), (pb_from, pb), (mine_from, mine), (wqkv_from, wqkv))
        )
    ]
    ys = Halving(at, y_bufs, y_sem, [[0, 1, 2], [1, 2, 0], [2, 0, 1]])
    half_loads = [
        pltpu.make_async_copy(y_far, y_bufs[0], load_sem.at[0]),
        pltpu.make_async_copy(y_half, kept, load_sem.at[1]),
    ]
    for copy in loads + half_loads:
        copy.start()

    span = 2 * rows
    met()

    homes = [
        Homeward(
            at, tiles, t + 1, both_g.at[t], down_g.at[t], in_parts, down_parts, weight_sem.at[t], down_sem.at[t]
        )
        for t in range(2)
    ]
    homes[0].start()
    n1_copy = pltpu.make_async_copy(n1_in, n1, n1_sem.at[0])

    lane = lane_of((rows, 128))
    comb_rows = []
    for e in range(exps):
        total = c_in[e]
        for q in range(1, QUAD):
            total = total + c_in[q * exps + e]
        comb_rows.append(total[0:1, :])
    comb_rows.append(jnp.zeros((128 - exps, rows), full))
    comb_grad = jnp.concatenate(comb_rows, axis=0).T
    valid = row_of((rows, 1)) < lengths[at.me]
    probs = probs_in[...]
    hot = routed(routes_t, at.me, rows)
    picked = jnp.where(hot, probs, 0.0)
    total = jnp.sum(picked, axis=1, keepdims=True)
    gate = picked / total
    gate_grad_rows = jnp.where(valid, comb_grad, 0.0)
    spread_grad = jnp.sum(gate_grad_rows * gate, axis=1, keepdims=True)
    probs_grad = jnp.where(hot, (gate_grad_rows - spread_grad) / total, 0.0)
    logit_grad = probs * (probs_grad - jnp.sum(probs_grad * probs, axis=1, keepdims=True))
    small_rows = small_send.shape[0]
    small_send[...] = jnp.zeros_like(small_send)
    router_back = jnp.dot(
        logit_grad, jnp.concatenate([router, jnp.zeros((128 - exps, width), full)], axis=0),
        precision=highest, preferred_element_type=full,
    )
    for copy in loads:
        copy.wait()
    h1 = h1_in[...]
    r2 = lax.rsqrt(jnp.mean(h1 * h1, axis=1, keepdims=True) + eps_norm)

    steps = len(ys.chip_bits)
    n2_grad = router_back + n_total[...].astype(full)
    scaled = n2_grad * gains[1:2, :]
    cot_copy.wait()
    dealt = deal[at.me] - at.base
    g = dn1_send[0]
    for e in range(1, exps):
        g = jnp.where(dealt == e, dn1_send[e], g)
    hidden_grad = (
        jnp.where(valid, g.astype(full), 0.0)
        + r2 * scaled
        - h1 * (r2 * r2 * r2) * jnp.mean(scaled * h1, axis=1, keepdims=True)
    )
    dh1[...] = hidden_grad
    small_send[exps + 1 : exps + 2, :] = jnp.sum(n2_grad * h1 * r2, axis=0, keepdims=True)
    branch = hidden_grad.astype(low)
    dz_send[...] = branch
    for e in range(exps):
        total = jnp.zeros((rows, row_block), full)
        for r in range(reps):
            total = total + nt(branch[:, r * out_cols : (r + 1) * out_cols], wout[e, r])
        do_send[e] = total.astype(low)

    def do_copies():
        return [
            send(
                do_send.at[exp_peer(k)],
                do_in.at[at.exp],
                do_sem.at[SEND, exp_peer(k)],
                do_sem.at[RECV, at.exp],
                at.device(at.rep, exp_peer(k)),
            )
            for k in range(1, exps)
        ]

    for copy in do_copies():
        copy.start()
    pltpu.make_async_copy(do_send.at[at.exp], do_in.at[at.exp], do_sem.at[RECV, at.exp]).start()

    group_dz = Group(at, dz_send, dz_all, dz_sem)
    dz_all[at.exp] = branch
    for copy in half_loads:
        copy.wait()

    def add_halves(j, _):
        y_bufs[0][j] = y_bufs[0][j] + kept[j]
        return 0

    lax.fori_loop(0, kept.shape[0], add_halves, 0)
    n1_copy.start()

    bias_sum[...] = jnp.zeros_like(bias_sum)

    def dn1_copies():
        beside, across = turn(at.exp, 2), turn(at.exp, 1)
        return [
            functools.partial(
                send, dn1_send.at[k], dn1_in.at[j], dn1_sem.at[SEND, j], dn1_sem.at[RECV, j], at.device(at.rep, to)
            )
            for k, j, to in ((turn(at.exp, 0), 2, beside), (across, 0, across), (beside, 1, beside))
        ]

    def attend_back(i, _):
        s = turn(at.exp, i)
        arrived(do_in.at[s], do_sem.at[RECV, s])

        @pl.when(i == 0)
        def _():
            group_dz.start()
            ys.start(0)

        @pl.when(i == 2)
        def _():
            group_dz.pass_on()

        block_lane = lane_of((rows, block_cols))
        for c in range(head_cols // block_cols):
            cols = slice(c * block_cols, (c + 1) * block_cols)
            k_cols = slice(head_cols + c * block_cols, head_cols + (c + 1) * block_cols)
            v_cols = slice(2 * head_cols + c * block_cols, 2 * head_cols + (c + 1) * block_cols)
            q = qkv[s, :, cols] * scale
            k = qkv[s, :, k_cols]
            v = qkv[s, :, v_cols]
            do = do_in[s, :, cols]
            dq = jnp.zeros((rows, block_cols), full)
            dk = jnp.zeros((rows, block_cols), full)
            dv = jnp.zeros((rows, block_cols), full)
            for t in range(block_cols // head_dim):
                h = c * (block_cols // head_dim) + t
                here = jnp.logical_and(block_lane >= t * head_dim, block_lane < (t + 1) * head_dim)
                zero = jnp.zeros_like(q)
                do_h = jnp.where(here, do, zero)
                weights = pb[s * heads + h]
                p = weights.astype(full)
                dp = nt(do_h, v)
                delta = jnp.sum(dp * p, axis=1, keepdims=True)
                ds = (p * (dp - delta)).astype(low)
                bias_sum[h] += ds.astype(full)
                dv = jnp.where(here, tn(weights, do), dv)
                dq = jnp.where(here, jnp.dot(ds, k, preferred_element_type=full), dq)
                dk = jnp.where(here, tn(ds, q), dk)
            dqkv[:, cols] = (dq * scale).astype(low)
            dqkv[:, k_cols] = dk.astype(low)
            dqkv[:, v_cols] = dv.astype(low)
        dqkv_t[:, pl.ds(pl.multiple_of(s * rows, rows), rows)] = dqkv[...].T
        for e in range(exps):
            dn1_send[s, :, e * row_block : (e + 1) * row_block] = jnp.dot(
                dqkv[...], wqkv[e], preferred_element_type=full
            ).astype(low)

        @pl.when(i == 0)
        def _():
            dn1_copies()[0]().start()

        @pl.when(i == 1)
        def _():
            arrived(dn1_in.at[2], dn1_sem.at[RECV, 2])
            dn1_send[s] = (dn1_send[s].astype(full) + dn1_in[2].astype(full)).astype(low)
            dn1_copies()[1]().start()

        @pl.when(i == 2)
        def _():
            dn1_copies()[2]().start()

        return 0

    lax.fori_loop(0, exps, attend_back, 0)

    n1_copy.wait()
    seg = wq_send.shape[2]
    parts = wq_send.shape[1]
    segs = mids.shape[1] - 1
    for e in range(exps):
        part = kept[0:exps, :, e * row_block : (e + 1) * row_block].reshape(exps * rows, row_block)
        total = dot(dqkv_t[...], part)
        for j in range(parts):
            wq_send[e, j] = total[j * seg : (j + 1) * seg].astype(low)

    def owner(j):
        section, within = j // (head_cols // seg), j % (head_cols // seg)
        col = section * width + at.exp * head_cols + within * seg
        block = col // seg
        return block // segs, block % segs

    def mid_place(grp, k, quad):
        return (grp * (segs + 1) + k) * QUAD + quad

    def mid_copy(src, send_sem, rep, k, e):
        dst = mids.at[rep // QUAD, k, at.quad]
        recv = mid_sem.at[mid_place(rep // QUAD, k, at.quad)]
        stays = jnp.logical_and(rep % QUAD == at.quad, e == at.exp)
        return (
            stays,
            functools.partial(send, src, dst, send_sem, recv, (at.grp, rep % QUAD, e)),
            functools.partial(pltpu.make_async_copy, src, dst, recv),
        )

    def wq_copy(i):
        e, j = i // parts, i % parts
        rep, k = owner(j)
        return mid_copy(wq_send.at[e, j], wq_sem.at[i], rep, k, e)

    def og_copy(r):
        return mid_copy(og_send.at[r], og_sem.at[r], r, segs, at.exp)

    def go(copies, act, act_local):
        stays, away, local = copies

        @pl.when(jnp.logical_not(stays))
        def _():
            act(away)

        if act_local:

            @pl.when(stays)
            def _():
                act_local(local)

    def over(count, copies, act, act_local):
        def one(i, _):
            go(copies(i), act, act_local)
            return 0

        lax.fori_loop(0, count, one, 0)

    over(exps * parts, wq_copy, lambda copy: copy().start(), lambda copy: copy().start())
    group_dz.arrive()
    grad = tn(mine[...].reshape(exps * rows, head_cols), dz_all[...].reshape(exps * rows, width))
    for r in range(reps):
        og_send[r] = grad[:, r * out_cols : (r + 1) * out_cols].T.astype(low)
    over(reps, og_copy, lambda copy: copy().start(), lambda copy: copy().start())
    ys.next(0)
    homes[1].start()

    n1_grad = dn1_send[at.exp].astype(full)
    for j in range(2):
        arrived(dn1_in.at[j], dn1_sem.at[RECV, j])
        n1_grad = n1_grad + dn1_in[j].astype(full)
    x = tokens[...].astype(full)
    r1 = lax.rsqrt(jnp.mean(x * x, axis=1, keepdims=True) + eps_norm)
    scaled = n1_grad * gains[0:1, :]
    token_grad[...] = (
        dh1[...] + r1 * scaled - x * (r1 * r1 * r1) * jnp.mean(scaled * x, axis=1, keepdims=True)
    )
    small_send[exps : exps + 1, :] = jnp.sum(n1_grad * x * r1, axis=0, keepdims=True)

    ys.next(1)
    router_rows = lax.dot_general(
        logit_grad, n2_in[...].astype(full), (((0,), (0,)), ((), ())), preferred_element_type=full, precision=highest
    )
    small_send[0:exps, :] = router_rows[0:exps, :]

    flip = jnp.where(row_of((rows, rows)) + lane_of((rows, rows)) == rows - 1, 1.0, 0.0).astype(low)
    diagonals = []
    for h in range(heads):
        high = bias_sum[h].astype(low)
        rest = (bias_sum[h] - high.astype(full)).astype(low)
        flipped = dot(high, flip) + dot(rest, flip)
        square = jnp.concatenate([flipped, jnp.zeros((rows, rows), full)], axis=1)
        turned = pltpu.roll(square, 0, 1, stride=1, stride_axis=0)
        diagonals.append(jnp.sum(turned, axis=0, keepdims=True))
    diagonals = jnp.concatenate(diagonals + [jnp.zeros((8 - heads, span), full)], axis=0)
    in_bucket = jnp.where(bucket_of(rows - 1 - row_of((span, 128))) == lane_of((span, 128)), 1.0, 0.0)
    bias_line = jnp.dot(diagonals, in_bucket, precision=highest, preferred_element_type=full)
    for h in range(heads):
        small_send[exps + 2 : exps + 3, h * 128 : (h + 1) * 128] = bias_line[h : h + 1, :]

    def small_copies():
        return [
            send(
                small_send,
                small_exp.at[at.exp],
                small_sem.at[SEND, exp_peer(k)],
                small_sem.at[RECV, at.exp],
                at.device(at.rep, exp_peer(k)),
            )
            for k in range(1, exps)
        ]

    for copy in small_copies():
        copy.start()
    small_exp[at.exp] = small_send[...]

    def mid_sum(grp, k):
        for q in range(QUAD):
            arrived(mids.at[grp, k, q], mid_sem.at[mid_place(grp, k, q)])
        total = mids[grp, k, 0].astype(full)
        for q in range(1, QUAD):
            total = total + mids[grp, k, q].astype(full)
        return total

    far = 1 - at.grp
    for k in range(segs + 1):
        far_send[k] = mid_sum(far, k).astype(low)

    def far_copy():
        return send(far_send, far_in, far_sem.at[SEND], far_sem.at[RECV], (far, at.quad, at.exp))

    far_copy().start()
    for k in range(1, exps):
        arrived(small_exp.at[exp_peer(k)], small_sem.at[RECV, exp_peer(k)])
    total = small_exp[0]
    for e in range(1, exps):
        total = total + small_exp[e]
    small_sum[...] = total
    for e in range(exps):
        small_sum[exps + 3 + e : exps + 4 + e, :] = small_exp[e, exps + 2 : exps + 3, :]

    def small2_copies():
        return [
            send(
                small_sum,
                small_rep.at[at.quad],
                small2_sem.at[SEND, k - 1],
                small2_sem.at[RECV, at.quad],
                (at.grp, (at.quad + k) % QUAD, at.exp),
            )
            for k in range(1, QUAD)
        ]

    def small3_copy():
        return send(small_half, small_far, small3_sem.at[SEND], small3_sem.at[RECV], (far, at.quad, at.exp))

    for copy in small2_copies():
        copy.start()
    small_rep[at.quad] = small_sum[...]
    for step in range(2, steps):
        ys.next(step)
    length = lengths[at.base]
    for e in range(1, exps):
        length = jnp.where(deal[at.base + e] == at.me, lengths[at.base + e], length)
    block = ys.result()[0]
    block_out[...] = jnp.where(row_of((rows, 1)) < length, block, jnp.zeros_like(block))
    for k in range(1, QUAD):
        arrived(small_rep.at[(at.quad + k) % QUAD], small2_sem.at[RECV, (at.quad + k) % QUAD])
    total = small_rep[0]
    for q in range(1, QUAD):
        total = total + small_rep[q]
    small_half[...] = total
    small3_copy().start()
    arrived(small_far, small3_sem.at[RECV])
    total = small_half[...] + small_far[...]
    small_out[...] = total

    near = [mid_sum(at.grp, k) for k in range(segs + 1)]
    arrived(far_in, far_sem.at[RECV])
    grads = [(near[k] + far_in[k].astype(full)).T for k in range(segs + 1)]
    qkv_grad[...] = jnp.concatenate(grads[:segs], axis=1)
    out_grad[...] = grads[segs]
    for home in homes:
        home.arrive()

    ys.finish()

    for home in homes:
        home.sent()

    over(exps * parts, wq_copy, lambda copy: copy().wait_send(), None)
    over(reps, og_copy, lambda copy: copy().wait_send(), None)
    far_copy().wait_send()
    small3_copy().wait_send()
    for copies in (do_copies(), small_copies(), small2_copies()):
        for copy in copies:
            copy.wait_send()
    for copy in dn1_copies():
        copy().wait_send()
    group_dz.sent()


def routed(routes_t, seq, rows):
    pair = routes_t[:, pl.ds(pl.multiple_of(seq * rows, rows), rows)].astype(full)
    cols = jnp.concatenate([pair, jnp.zeros((126, rows), full)], axis=0).T
    lane = lane_of((rows, 128)).astype(full)
    return jnp.logical_or(lane == cols[:, 0:1], lane == cols[:, 1:2])


def backward_call(
    grps, exps, lengths, deal, y_half, y_far, both_g, down_g, in_before, down_before, n1,
    cot_all, routes_t, tokens, n_total, c_in, n2, probs, h1, qkv, pb, mine, wqkv, wout, gains, router
):
    reps = grps * QUAD
    rows, width = tokens.shape
    heads = HEADS // exps
    head_cols = width // exps
    row_block = wqkv.shape[2]
    out_cols = wout.shape[3]
    shard_cols = 3 * width // reps
    seg = math.gcd(shard_cols, head_cols)
    segs = shard_cols // seg
    parts = 3 * head_cols // seg
    members = QUAD * exps
    chip_bits = bits_of(members) - 1
    small_rows = -(-(2 * exps + 3) // 8) * 8
    shape = jax.ShapeDtypeStruct
    vmem = pl.BlockSpec(memory_space=pltpu.VMEM)
    smem = pl.BlockSpec(memory_space=pltpu.SMEM)
    hbm = pl.BlockSpec(memory_space=pl.ANY)
    results = [
        (shape((rows, width), full), vmem),
        (shape((rows, width), low), vmem),
        (shape(in_before.shape, low), hbm),
        (shape(down_before.shape, low), hbm),
        (shape((row_block, shard_cols), full), vmem),
        (shape((row_block, out_cols), full), vmem),
        (shape((small_rows, width), full), vmem),
    ]
    dma = pltpu.SemaphoreType.DMA
    bufs = [pltpu.VMEM((1 << (chip_bits - s), rows, width), low) for s in range(chip_bits + 1)]
    return pl.pallas_call(
        functools.partial(backward_kernel, grps, exps),
        out_shape=[r[0] for r in results],
        in_specs=[smem] * 2 + [hbm] * 8 + [vmem] * 6 + [hbm] * 6 + [vmem] * 2,
        out_specs=[r[1] for r in results],
        scratch_shapes=[
            pltpu.VMEM(h1.shape, full),
            pltpu.VMEM(qkv.shape, low),
            pltpu.VMEM(pb.shape, low),
            pltpu.VMEM(mine.shape, low),
            pltpu.VMEM(wqkv.shape, low),
            pltpu.VMEM(wout.shape, low),
            pltpu.VMEM((members // 2, rows, width), low),
            list(bufs),
            pltpu.VMEM((rows, width), full),
            pltpu.VMEM((rows, width), low),
            pltpu.VMEM((exps, rows, width), low),
            pltpu.VMEM((exps, rows, head_cols), low),
            pltpu.VMEM((exps, rows, head_cols), low),
            pltpu.VMEM((heads, rows, rows), full),
            pltpu.VMEM((rows, 3 * head_cols), low),
            pltpu.VMEM((3 * head_cols, exps * rows), low),
            pltpu.VMEM((exps, rows, width), low),
            pltpu.VMEM((3, rows, width), low),
            pltpu.VMEM((exps, parts, seg, row_block), low),
            pltpu.VMEM((reps, seg, row_block), low),
            pltpu.VMEM((grps, segs + 1, QUAD, seg, row_block), low),
            pltpu.VMEM((segs + 1, seg, row_block), low),
            pltpu.VMEM((segs + 1, seg, row_block), low),
            pltpu.VMEM((small_rows, width), full),
            pltpu.VMEM((exps, small_rows, width), full),
            pltpu.VMEM((small_rows, width), full),
            pltpu.VMEM((QUAD, small_rows, width), full),
            pltpu.VMEM((small_rows, width), full),
            pltpu.VMEM((small_rows, width), full),
            dma((2, 3 << chip_bits)),
            dma((2,)),
            dma((2, 2, 2 * reps)),
            dma((2, 2, max(QUAD, grps))),
            dma((2, exps)),
            dma((2, exps)),
            dma((2, exps)),
            dma((exps * parts,)),
            dma((reps,)),
            dma((grps * (segs + 1) * QUAD,)),
            dma((2,)),
            dma((2, exps)),
            dma((2, QUAD)),
            dma((2,)),
            dma((2,)),
            dma((6,)),
        ],
        compiler_params=pltpu.CompilerParams(
            collective_id=1, has_side_effects=True, vmem_limit_bytes=60 * 1024 * 1024
        ),
        input_output_aliases={6: 2, 7: 3},
        name="backward",
    )(
        lengths, deal, y_half, y_far, both_g, down_g, in_before, down_before, n1, cot_all,
        routes_t, tokens, n_total, c_in, n2, probs, h1, qkv, pb, mine, wqkv, wout, gains, router
    )


def per_device(
    tokens,
    cotangent,
    seq_lengths,
    deal,
    routes,
    attn_qkv,
    qkv_first,
    qkv_second,
    attn_out,
    out_first,
    out_second,
    rel_bias,
    bias_first,
    bias_second,
    router,
    router_first,
    router_second,
    norm_gains,
    gains_first,
    gains_second,
    expert_in,
    in_first,
    in_second,
    expert_out,
    down_first,
    down_second,
):
    rows, width = tokens.shape
    experts = router.shape[1]
    capacity = (10 * rows + 4 * experts - 1) // (4 * experts)
    exps = lax.axis_size("exp")
    grps = lax.axis_size("grp")
    routes_t = routes.T
    bias_table = rel_bias.T
    (
        both_w, down_w, cot_all, n_all, comb_all, qkv, pb, context_mine, normed_group, wqkv, wout, hidden_one,
        normed_two, router_probs, in_low, down_low,
    ) = forward_call(
        grps, exps, seq_lengths, bias_table, routes_t, tokens, cotangent, norm_gains.T, router.T,
        attn_qkv, attn_out, expert_in[0], expert_out[0],
    )
    n_total, y_half, y_far, c_in, both_g, down_g, in_before, down_before = expert_call(
        grps, exps, capacity, deal, routes_t, comb_all, n_all, cot_all, both_w, down_w, in_low, down_low,
        hidden_one,
    )
    token_grad, block_out, in_parts, down_parts, qkv_grad, out_grad, small = backward_call(
        grps, exps, seq_lengths, deal, y_half, y_far, both_g, down_g,
        in_before, down_before, normed_group, cot_all, routes_t, tokens, n_total, c_in, normed_two, router_probs, hidden_one, qkv, pb, context_mine, wqkv,
        wout, norm_gains.T, router.T,
    )
    states = [
        attn_qkv, qkv_first, qkv_second, attn_out, out_first, out_second, bias_table, bias_first.T, bias_second.T,
        router.T, router_first.T, router_second.T, norm_gains.T, gains_first.T, gains_second.T,
        expert_in[0], in_first[0], in_second[0], expert_out[0], down_first[0], down_second[0],
    ]
    new = list(adam_call(exps, in_parts, down_parts, qkv_grad, out_grad, small, states))
    new = new[:6] + [array.T for array in new[6:15]] + [array[None] for array in new[15:]]
    return (block_out, token_grad, *new)


def bucket_onehot(length):
    places = jnp.arange(length, dtype=jnp.int32)
    offset = places[None, :] - places[:, None]
    distance = jnp.abs(offset)
    bucket = 16 * (offset > 0).astype(jnp.int32)
    for threshold in thresholds:
        bucket = bucket + (distance >= threshold).astype(jnp.int32)
    return (bucket[:, :, None] == jnp.arange(BUCKETS, dtype=jnp.int32)[None, None, :]).astype(full)


def swap(pieces, axes):
    return lax.all_to_all(pieces, axes, split_axis=0, concat_axis=0, tiled=True)


def spread(block, axes):
    members = lax.axis_size(axes)
    return swap(jnp.broadcast_to(block[None], (members,) + block.shape), axes)


def plain_device(
    tokens,
    cotangent,
    seq_lengths,
    deal,
    routes,
    attn_qkv,
    qkv_first,
    qkv_second,
    attn_out,
    out_first,
    out_second,
    rel_bias,
    bias_first,
    bias_second,
    router,
    router_first,
    router_second,
    norm_gains,
    gains_first,
    gains_second,
    expert_in,
    in_first,
    in_second,
    expert_out,
    down_first,
    down_second,
):
    rows, width = tokens.shape
    head_dim = width // HEADS
    score_scale = 1.0 / math.sqrt(head_dim)
    experts = router.shape[1]
    capacity = (10 * rows + 4 * experts - 1) // (4 * experts)
    exps = lax.axis_size("exp")
    grps = lax.axis_size("grp")
    reps = grps * QUAD
    heads = HEADS // exps
    head_cols = heads * head_dim
    place = lax.axis_index("exp")
    base = lax.axis_index(REP) * exps
    me = base + place
    slab = expert_in.shape[1]
    units = expert_out.shape[1]
    quarter = grps * units

    row_block = attn_qkv.shape[0]
    qkv_rows = lax.all_gather(attn_qkv.astype(low), REP, axis=1, tiled=True)
    out_rows = lax.all_gather(attn_out.astype(low), REP, axis=1, tiled=True)
    qkv_pieces = jnp.transpose(
        qkv_rows.reshape(row_block, 3, exps, head_cols), (2, 0, 1, 3)
    ).reshape(exps, row_block, 3 * head_cols)
    qkv_mine = swap(qkv_pieces, "exp").reshape(width, 3 * head_cols)
    full_out = spread(out_rows, "exp").reshape(width, width)

    group_tokens = spread(tokens, "exp")
    group_cotangent = spread(cotangent, "exp")
    my_cotangent = lax.dynamic_index_in_dim(group_cotangent, deal[me] - base, 0, keepdims=False)

    my_routes = lax.dynamic_slice_in_dim(routes, me * rows, rows, 0)
    places = jnp.arange(rows, dtype=jnp.int32)
    valid_rows = (places < seq_lengths[me]).astype(full)
    group_lengths = lax.dynamic_slice_in_dim(seq_lengths, base, exps, 0)
    key_ok = places[None, :] < group_lengths[:, None]
    gain_one = norm_gains[:, 0]
    gain_two = norm_gains[:, 1]

    chosen = (my_routes[:, :, None] == jnp.arange(experts, dtype=jnp.int32)[None, None, :]).astype(full)
    flat_routes = my_routes.reshape(-1)
    route_hot = (flat_routes[:, None] == jnp.arange(experts, dtype=jnp.int32)[None, :]).astype(jnp.int32)
    before = jnp.cumsum(route_hot, axis=0) - route_hot
    slot_index = jnp.sum(before * route_hot, axis=-1)
    target = (flat_routes * capacity + slot_index).reshape(rows, 2)
    slots = experts * capacity
    slot_ids = jnp.arange(slots, dtype=jnp.int32)
    place_first = slot_ids[:, None] == target[None, :, 0]
    place_second = slot_ids[:, None] == target[None, :, 1]
    place_any = jnp.logical_or(place_first, place_second).astype(low)

    shard_in = expert_in[0].astype(low).reshape(slab, 2, grps, QUAD, units)
    in_pieces = jnp.transpose(shard_in, (1, 3, 0, 2, 4)).reshape(2, 1, QUAD, slab, quarter)
    in_pieces = jnp.broadcast_to(in_pieces, (2, grps, QUAD, slab, quarter)).reshape(
        2, reps, slab, quarter
    )
    down_mine = spread(expert_out[0].astype(low), "grp").reshape(quarter, width)
    gate_mine = swap(in_pieces[0], REP).reshape(width, quarter)
    up_mine = swap(in_pieces[1], REP).reshape(width, quarter)

    upstream = my_cotangent.astype(full) * valid_rows[:, None]

    def to_experts(block):
        sent = block.reshape((1, experts) + block.shape[1:])
        sent = jnp.broadcast_to(sent, (QUAD,) + sent.shape[1:])
        return swap(sent.reshape((QUAD * experts,) + block.shape[1:]), PLANE)

    def dispatch(values):
        return dot(place_any, values).astype(low).reshape(experts, capacity, width)

    expert_upstream = to_experts(dispatch(upstream.astype(low))).reshape(-1, width)
    active_grad_bare = lax.dot_general(
        expert_upstream, down_mine, (((1,), (1,)), ((), ())), preferred_element_type=full
    )

    x_group = group_tokens.astype(full)
    scale_group = lax.rsqrt(jnp.mean(x_group * x_group, axis=-1, keepdims=True) + eps_norm)
    normed_group = (x_group * scale_group * gain_one).astype(low).reshape(exps * rows, width)
    qkv = dot(normed_group, qkv_mine).astype(low).reshape(exps, rows, 3, heads, head_dim)
    queries = qkv[:, :, 0]
    key_rows = qkv[:, :, 1]
    values = qkv[:, :, 2]
    onehot = bucket_onehot(rows)
    bias_mine = lax.dynamic_slice_in_dim(rel_bias, place * heads, heads, 1)
    bias_table = jnp.einsum("ijb,bh->hij", onehot, bias_mine, precision=highest)

    def scores_of():
        raw = (
            jnp.einsum("sihd,sjhd->shij", queries, key_rows, preferred_element_type=full)
            * score_scale
            + bias_table[None]
        )
        return jnp.where(key_ok[:, None, None, :], raw, -1e30)

    scores = scores_of()
    row_max = jnp.max(scores, axis=-1, keepdims=True)
    log_total = row_max + jnp.log(jnp.sum(jnp.exp(scores - row_max), axis=-1, keepdims=True))
    weights_low = jnp.exp(scores - log_total).astype(low)
    context_mine = (
        jnp.einsum("shij,sjhd->sihd", weights_low, values, preferred_element_type=full)
        .astype(low)
        .reshape(exps, rows, head_cols)
    )
    context = jnp.transpose(swap(context_mine, "exp"), (1, 0, 2)).reshape(rows, width)

    x_float = tokens.astype(full)
    scale_one = lax.rsqrt(jnp.mean(x_float * x_float, axis=-1, keepdims=True) + eps_norm)
    hidden_one = x_float + dot(context, full_out)
    scale_two = lax.rsqrt(jnp.mean(hidden_one * hidden_one, axis=-1, keepdims=True) + eps_norm)
    normed_two = (hidden_one * scale_two * gain_two).astype(low)
    normed_float = normed_two.astype(full)
    router_probs = jax.nn.softmax(jnp.dot(normed_float, router, precision=highest), axis=-1)
    picked = jnp.sum(router_probs[:, None, :] * chosen, axis=-1)
    gate_total = jnp.sum(picked, axis=-1, keepdims=True)
    gate_value = picked / gate_total
    combine = gate_value * valid_rows[:, None]
    combine_slots = jnp.sum(
        jnp.where(place_first, combine[None, :, 0], 0.0)
        + jnp.where(place_second, combine[None, :, 1], 0.0),
        axis=1,
    ).reshape(experts, 1, capacity)

    expert_rows = to_experts(dispatch(normed_two)).reshape(-1, width)
    expert_combine = to_experts(combine_slots).reshape(-1, 1)

    gate_part = dot(expert_rows, gate_mine)
    up_part = dot(expert_rows, up_mine)
    active_float, active_pull = jax.vjp(gated_unit, gate_part, up_part)
    active = active_float.astype(low)
    active_scaled = (active_float * expert_combine).astype(low)
    combine_grad_part = jnp.sum(active_float * active_grad_bare, axis=-1).reshape(
        QUAD * experts, 1, capacity
    )
    gate_part_grad, up_part_grad = active_pull(active_grad_bare * expert_combine)
    gate_part_grad = gate_part_grad.astype(low)
    up_part_grad = up_part_grad.astype(low)
    rows_grad_part = (
        lax.dot_general(gate_part_grad, gate_mine, (((1,), (1,)), ((), ())), preferred_element_type=full)
        + lax.dot_general(up_part_grad, up_mine, (((1,), (1,)), ((), ())), preferred_element_type=full)
    ).astype(low)
    output_part = dot(active, down_mine).astype(low)

    combine_grad_back = swap(combine_grad_part, PLANE)
    rows_grad_back = swap(rows_grad_part.reshape(QUAD * experts, capacity, width), PLANE)
    output_back = swap(output_part.reshape(QUAD * experts, capacity, width), PLANE)

    def transposed_dot(a, b):
        return lax.dot_general(a, b, (((0,), (0,)), ((), ())), preferred_element_type=full)

    down_grad = transposed_dot(active_scaled, expert_upstream).astype(low)
    gate_grad = transposed_dot(expert_rows, gate_part_grad).astype(low)
    up_grad = transposed_dot(expert_rows, up_part_grad).astype(low)
    down_share = jnp.sum(
        swap(down_grad.reshape(grps, units, width), "grp").astype(full), axis=0
    )[None]

    def in_columns(grad):
        back = swap(grad.reshape(reps, slab, quarter), REP).astype(full)
        back = jnp.sum(back.reshape(grps, QUAD, slab, grps, units), axis=0)
        return jnp.transpose(back, (1, 2, 0, 3)).reshape(slab, grps * QUAD * units)

    in_share = jnp.concatenate([in_columns(gate_grad), in_columns(up_grad)], axis=1)[None]

    def from_slots(placed, parts):
        hot = jnp.broadcast_to(placed.astype(low)[None], (QUAD,) + placed.shape).reshape(-1, rows)
        return lax.dot_general(
            hot, parts.reshape(-1, width), (((0,), (0,)), ((), ())), preferred_element_type=full
        )

    mixture = combine[:, :1] * from_slots(place_first, output_back) + combine[:, 1:] * from_slots(
        place_second, output_back
    )
    block_loader = (valid_rows[:, None] * (hidden_one + mixture)).astype(low)
    seq_ids = jnp.arange(deal.shape[0], dtype=jnp.int32)
    dealt_seq = jnp.sum(jnp.where(deal == me, seq_ids, 0))
    block_out = lax.dynamic_index_in_dim(
        spread(block_loader, "exp"), dealt_seq - base, 0, keepdims=False
    )

    combine_grad_slots = jnp.sum(combine_grad_back.reshape(QUAD, slots), axis=0)
    combine_grad = jnp.stack(
        [
            jnp.sum(jnp.where(place_first, combine_grad_slots[:, None], 0.0), axis=0),
            jnp.sum(jnp.where(place_second, combine_grad_slots[:, None], 0.0), axis=0),
        ],
        axis=1,
    )
    gate_grad_value = combine_grad * valid_rows[:, None]
    picked_grad = (
        gate_grad_value - jnp.sum(gate_grad_value * gate_value, axis=-1, keepdims=True)
    ) / gate_total
    probs_grad = jnp.sum(picked_grad[:, :, None] * chosen, axis=1)
    logit_grad = router_probs * (
        probs_grad - jnp.sum(probs_grad * router_probs, axis=-1, keepdims=True)
    )
    router_grad = jnp.dot(normed_float.T, logit_grad, precision=highest)
    normed_grad = jnp.dot(logit_grad, router.T, precision=highest) + from_slots(
        jnp.logical_or(place_first, place_second), rows_grad_back
    )
    scaled_two = normed_grad * gain_two
    hidden_grad = (
        upstream
        + scale_two * scaled_two
        - hidden_one * scale_two**3 * jnp.mean(scaled_two * hidden_one, axis=-1, keepdims=True)
    )
    gain_two_grad = jnp.sum(normed_grad * hidden_one * scale_two, axis=0)
    branch_grad = hidden_grad.astype(low)
    context_grad = lax.dot_general(
        branch_grad, full_out, (((1,), (1,)), ((), ())), preferred_element_type=full
    ).astype(low)
    context_grad_pieces = jnp.transpose(context_grad.reshape(rows, exps, head_cols), (1, 0, 2))
    context_grad_mine = swap(context_grad_pieces, "exp").reshape(exps, rows, heads, head_dim)
    branch_group = spread(branch_grad, "exp").reshape(exps * rows, width)
    out_grad = transposed_dot(context_mine.reshape(exps * rows, head_cols), branch_group).astype(low)

    scores = scores_of()
    probs_again = jnp.exp(scores - log_total)
    weights_again = probs_again.astype(low)
    values_grad = jnp.einsum(
        "shij,sihd->sjhd", weights_again, context_grad_mine, preferred_element_type=full
    )
    probs_grad_att = jnp.einsum(
        "sihd,sjhd->shij", context_grad_mine, values, preferred_element_type=full
    )
    row_delta = jnp.sum(probs_grad_att * probs_again, axis=-1, keepdims=True)
    scores_grad = (probs_again * (probs_grad_att - row_delta)).astype(low)
    scores_grad_sum = jnp.sum(scores_grad.astype(full), axis=0)
    bias_grad_mine = jnp.einsum("hij,ijb->bh", scores_grad_sum, onehot, precision=highest)
    bias_grad = lax.dynamic_update_slice_in_dim(
        jnp.zeros((BUCKETS, HEADS), full), bias_grad_mine, place * heads, 1
    )
    queries_grad = (
        jnp.einsum("shij,sjhd->sihd", scores_grad, key_rows, preferred_element_type=full)
        * score_scale
    )
    keys_grad = (
        jnp.einsum("shij,sihd->sjhd", scores_grad, queries, preferred_element_type=full)
        * score_scale
    )
    qkv_grad = (
        jnp.stack([queries_grad, keys_grad, values_grad], axis=2)
        .astype(low)
        .reshape(exps * rows, 3 * head_cols)
    )
    normed_one_part = lax.dot_general(
        qkv_grad, qkv_mine, (((1,), (1,)), ((), ())), preferred_element_type=full
    ).astype(low)
    normed_one_grad = jnp.sum(
        swap(normed_one_part.reshape(exps, rows, width), "exp").astype(full), axis=0
    )
    scaled_one = normed_one_grad * gain_one
    token_grad = (
        hidden_grad
        + scale_one * scaled_one
        - x_float * scale_one**3 * jnp.mean(scaled_one * x_float, axis=-1, keepdims=True)
    )
    gain_one_grad = jnp.sum(normed_one_grad * x_float * scale_one, axis=0)

    qkv_weight_grad = transposed_dot(normed_group, qkv_grad).astype(low)
    qkv_grad_rows = swap(qkv_weight_grad.reshape(exps, row_block, 3 * head_cols), "exp")
    qkv_grad_rows = jnp.transpose(
        qkv_grad_rows.reshape(exps, row_block, 3, head_cols), (1, 2, 0, 3)
    ).reshape(row_block, reps, -1)
    qkv_share = jnp.sum(
        swap(jnp.transpose(qkv_grad_rows, (1, 0, 2)), REP).astype(full), axis=0
    )
    out_pieces = jnp.transpose(out_grad.reshape(row_block, reps, -1), (1, 0, 2))
    out_share = jnp.sum(swap(out_pieces, REP).astype(full), axis=0)

    small = jnp.concatenate(
        [
            router_grad.reshape(-1),
            jnp.stack([gain_one_grad, gain_two_grad], axis=1).reshape(-1),
            bias_grad.reshape(-1),
        ]
    ).reshape(-1, 128)
    small_total = jnp.sum(lax.all_gather(small, ALL, axis=0, tiled=False), axis=0).reshape(-1)
    router_total = small_total[: router.size].reshape(router.shape)
    gains_total = small_total[router.size : router.size + norm_gains.size].reshape(norm_gains.shape)
    bias_total = small_total[router.size + norm_gains.size :].reshape(rel_bias.shape)

    qkv_new = adamw_update(attn_qkv, qkv_first, qkv_second, qkv_share, 1.5 / math.sqrt(D), 0.1)
    out_new = adamw_update(attn_out, out_first, out_second, out_share, 6.0 / math.sqrt(D), 0.1)
    bias_new = adamw_update(rel_bias, bias_first, bias_second, bias_total, 0.3, 0.0)
    router_new = adamw_update(
        router, router_first, router_second, router_total, 1.0 / math.sqrt(D), 0.1
    )
    gains_new = adamw_update(norm_gains, gains_first, gains_second, gains_total, 0.5, 0.0)
    in_new = adamw_update(expert_in, in_first, in_second, in_share, 1.5 / math.sqrt(D), 0.1)
    down_new = adamw_update(
        expert_out, down_first, down_second, down_share, 1.5 / math.sqrt(FF), 0.1
    )
    return (
        (block_out, token_grad)
        + qkv_new
        + out_new
        + bias_new
        + router_new
        + gains_new
        + in_new
        + down_new
    )


def solution(mesh):
    reps, exps = mesh.devices.shape
    split = Mesh(mesh.devices.reshape(reps // QUAD, QUAD, exps), ALL)
    by_rows = P(ALL, None)
    attn = P("exp", REP)
    expert = P("exp", REP, None)
    return jax.shard_map(
        per_device if (reps, exps) == (2 * QUAD, 4) else plain_device,
        mesh=split,
        in_specs=(by_rows, by_rows) + (P(),) * 3 + (attn,) * 6 + (P(),) * 9 + (expert,) * 6,
        out_specs=(by_rows, by_rows) + (attn,) * 6 + (P(),) * 9 + (expert,) * 6,
        check_vma=False,
    )
```
